32 devices in a mesh: mel: 4 (over y, x), tm: 8 (over z, core).
Axes of the slice: x: 2, y: 2, z: 4, core: 2. Of those that a mesh axis runs over, the one named last changes fastest.
Arguments:
- spectrum: bfloat16 [1, 64, 2048], P(None, 'mel', 'tm'), may hold values from -25 to 40
- clip_bounds: int32 [1, 4], replicated, may hold values from 0 to 2048, as said below
- kernel_one: bfloat16 [64, 3, 3], replicated, may hold values from -2 to 2
- gain_one: float32 [64], replicated, may hold values from 0.5 to 1.5
- bias_one: float32 [64], replicated, may hold values from -3 to 3
- kernel_two: bfloat16 [64, 64, 3, 3], replicated, may hold values from -0.25 to 0.25
- gain_two: float32 [64], replicated, may hold values from 0.5 to 1.5
- bias_two: float32 [64], replicated, may hold values from -3 to 3
- pooled_grad: bfloat16 [1, 64, 32, 1024], P(None, None, 'mel', 'tm'), may hold values from -14 to 19
Outputs:
- pooled: bfloat16 [1, 64, 32, 1024], P(None, None, 'mel', 'tm')
- spectrum_grad: float32 [1, 64, 2048], P(None, 'mel', 'tm')
- kernel_one_grad: float32 [64, 3, 3], replicated
- gain_one_grad: float32 [64], replicated
- bias_one_grad: float32 [64], replicated
- kernel_two_grad: float32 [64, 64, 3, 3], replicated
- gain_two_grad: float32 [64], replicated
- bias_two_grad: float32 [64], replicated
The draws below stay inside these ranges and needn't reach their ends.
Inputs may be any that keep to these rules, and one draw needn't show every extreme that they name: `clip_bounds`: in each row the entries rise strictly and are even; entry 0 is 0, entries 0 to 2 are the clips' first frames and entry 3 the end of the last clip; frames from there on are padding.
All inputs are finite; a program needn't handle non-finite values.
Results may differ from the reference program's by a relative error of at most 0.0056.
Values may be sent and summed in bfloat16 or wider, within the bound.
No kernel may reach another device: no remote copies, remote signals or barrier semaphores. Data moves between devices by JAX's collectives and lax.ppermute only.
A program may use at most 64 MiB of HBM per device.

```python
import jax
import jax.numpy as jnp
from jax import lax

MELS = 64
CH = 64
FD = 256
ROWS = 1
NSEG = 3
N_TM = 8


def draw_spectrum(key, part):
    key = jax.random.fold_in(key, 5)
    total = FD * N_TM
    key_base, key_mel = jax.random.split(key, 2)
    position = jnp.arange(total, dtype=jnp.float32) / total
    shape = (ROWS, MELS, total)
    base = 0.5 + jnp.clip(jax.random.normal(key_base, shape, jnp.float32), -3.0, 3.0)
    envelope = jnp.exp(jnp.log(3.0) * position)
    mel_scale = jnp.exp(jax.random.uniform(key_mel, (1, MELS, 1), jnp.float32, jnp.log(0.5), jnp.log(2.0)))
    return (base * envelope[None, None, :] * mel_scale).astype(jnp.bfloat16)


def draw_pooled_grad(key, part):
    key = jax.random.fold_in(key, 7)
    half = FD * N_TM // 2
    position = jnp.arange(half, dtype=jnp.float32) / half
    shape = (ROWS, CH, MELS // 2, half)
    base = 0.3 + jnp.clip(jax.random.normal(key, shape, jnp.float32), -4.0, 4.0)
    envelope = jnp.exp(jnp.log(3.0) * position)
    return (base * envelope[None, None, None, :]).astype(jnp.bfloat16)


def draw_clip_bounds(key, part):
    key = jax.random.fold_in(key, 11)
    total = FD * N_TM
    half = total // 2
    key_row, key_rest, key_tail = jax.random.split(key, 3)
    long_row = jax.random.randint(key_row, (), 0, ROWS)
    row_keys = jax.random.split(key_rest, ROWS)
    picks = jax.vmap(lambda row_key: jnp.sort(jax.random.permutation(row_key, half)[:NSEG]))(row_keys)
    general = ((picks + 1) * 2).astype(jnp.int32)
    tail = jnp.sort(jax.random.permutation(key_tail, FD // 2 - 1)[:NSEG - 1])
    tail_values = (total - FD + 2 + 2 * tail).astype(jnp.int32)
    long_values = jnp.concatenate([tail_values, jnp.array([total], jnp.int32)])
    chosen = jnp.where(jnp.arange(ROWS)[:, None] == long_row, long_values[None, :], general)
    return jnp.concatenate([jnp.zeros((ROWS, 1), jnp.int32), chosen], axis=1).astype(jnp.int32)


def gaussian(stream_key, dims, width, limit, held_as=jnp.bfloat16):
    values = width * jax.random.normal(stream_key, dims, jnp.float32)
    return jnp.clip(values, min=-limit, max=limit).astype(held_as)


def setup_inputs(seed: int = 0) -> dict:
    key_of = jax.random.split(jax.random.key(seed), 10)
    return {
        "spectrum": draw_spectrum(jax.random.fold_in(key_of[9], 71), 0),
        "clip_bounds": draw_clip_bounds(jax.random.fold_in(key_of[9], 71), 0),
        "kernel_one": gaussian(key_of[2], (CH, 3, 3), 9 ** -0.5, 2.0),
        "gain_one": jnp.clip(1.0 + 0.1 * jax.random.normal(key_of[3], (CH,), jnp.float32), 0.5, 1.5),
        "bias_one": gaussian(key_of[4], (CH,), 0.5, 3.0, jnp.float32),
        "kernel_two": gaussian(key_of[5], (CH, CH, 3, 3), (9 * CH) ** -0.5, 0.25),
        "gain_two": jnp.clip(1.0 + 0.1 * jax.random.normal(key_of[6], (CH,), jnp.float32), 0.5, 1.5),
        "bias_two": gaussian(key_of[7], (CH,), 0.5, 3.0, jnp.float32),
        "pooled_grad": draw_pooled_grad(jax.random.fold_in(key_of[9], 71), 0),
    }


@jax.custom_vjp
def low(v):
    return lax.optimization_barrier(v.astype(jnp.bfloat16)).astype(jnp.float32)

@jax.custom_vjp
def low_back(v):
    return v

def low_keep(v):
    return (low(v), None)

def low_pass(kept, grad):
    return (grad,)

def back_keep(v):
    return (v, None)

def back_low(kept, grad):
    return (low(grad),)
low.defvjp(low_keep, low_pass)
low_back.defvjp(back_keep, back_low)

def clip_masks(clip_bounds):
    total = FD * N_TM
    frames = jnp.arange(total, dtype=jnp.int32)
    starts = clip_bounds[:, :NSEG]
    clip_id = lax.optimization_barrier(jnp.sum((frames[None, :, None] >= starts[:, None, :]).astype(jnp.int32), axis=2))
    living = frames[None, :] < clip_bounds[:, NSEG:NSEG + 1]
    paired = living[:, :-1] & living[:, 1:] & (clip_id[:, :-1] == clip_id[:, 1:])
    paired = jnp.concatenate([paired, jnp.zeros((paired.shape[0], 1), dtype=bool)], axis=1)
    return (living.astype(jnp.float32), paired.astype(jnp.float32))

def convolve(field, kernel, paired):
    row_count, chan, mel_count, frame_count = field.shape
    padded = jnp.pad(field, ((0, 0), (0, 0), (1, 1), (1, 1)))
    behind = jnp.concatenate([jnp.zeros((row_count, 1), paired.dtype), paired[:, :-1]], axis=1)
    masks = [behind, jnp.ones_like(paired), paired]
    result = jnp.zeros((row_count, kernel.shape[0], mel_count, frame_count), jnp.float32)
    for frame_step in range(3):
        partial_sum = jnp.zeros_like(result)
        for mel_step in range(3):
            piece = padded[:, :, mel_step:mel_step + mel_count, frame_step:frame_step + frame_count]
            partial_sum = partial_sum + jnp.einsum('oc,rcmf->romf', kernel[:, :, mel_step, frame_step], piece, precision=lax.Precision.HIGHEST)
        result = result + partial_sum * masks[frame_step][:, None, None, :]
    return result

def batch_norm(field, gain, bias, usable4, pixel_count):
    total = lax.optimization_barrier(jnp.sum(field * usable4, axis=(0, 2, 3)))
    squares = lax.optimization_barrier(jnp.sum(field * field * usable4, axis=(0, 2, 3)))
    average = total / pixel_count
    variance = squares / pixel_count - average * average
    inv_std = lax.rsqrt(variance + 1e-05)
    return (field - average[None, :, None, None]) * (inv_std * gain)[None, :, None, None] + bias[None, :, None, None]

def reference(spectrum, clip_bounds, kernel_one, gain_one, bias_one, kernel_two, gain_two, bias_two, pooled_grad):
    usable, paired = clip_masks(clip_bounds)
    usable4 = usable[:, None, None, :]
    pixel_count = MELS * jnp.sum(usable)

    def forward(spec_float, first_kernel, first_gain, first_bias, second_kernel, second_gain, second_bias):
        masked_input = spec_float[:, None] * usable4
        pre_one = low_back(convolve(masked_input, first_kernel[:, None], paired))
        scaled_one = batch_norm(pre_one, first_gain, first_bias, usable4, pixel_count)
        act_one = low(jax.nn.silu(scaled_one) * usable4)
        pre_two = low_back(convolve(act_one, second_kernel, paired))
        scaled_two = batch_norm(pre_two, second_gain, second_bias, usable4, pixel_count)
        act_two = jax.nn.silu(scaled_two) * usable4
        row_count, chan, mel_count, frame_count = act_two.shape
        blocks = act_two.reshape(row_count, chan, mel_count // 2, 2, frame_count // 2, 2)
        return lax.optimization_barrier(jnp.mean(blocks, axis=(3, 5)))
    inputs = (spectrum.astype(jnp.float32), kernel_one.astype(jnp.float32), gain_one, bias_one, kernel_two.astype(jnp.float32), gain_two, bias_two)
    result, pullback = jax.vjp(forward, *inputs)
    grads = pullback(pooled_grad.astype(jnp.float32))
    return (result.astype(jnp.bfloat16), grads[0], grads[1], grads[2], grads[3], grads[4], grads[5], grads[6])
```

```python
import jax
import jax.numpy as jnp
from jax import lax
from jax.sharding import PartitionSpec as P


def with_halo(x, sides, width):
    for axis, dim in sides:
        size, length = (lax.axis_size(axis), x.shape[dim])
        up = [(i, (i + 1) % size) for i in range(size - 1)]
        down = [(j, i) for i, j in up]
        last = lax.slice_in_dim(x, length - width, length, axis=dim)
        leading = lax.slice_in_dim(x, 0, width, axis=dim)
        before = lax.ppermute(last, axis, up)
        after = lax.ppermute(leading, axis, down)
        x = jnp.concatenate([before, x, after], axis=dim)
    return x


def frame_masks(clip_bounds, frame_dev, margin):
    clip_total = clip_bounds.shape[1] - 1
    span = frame_dev + 2 * margin
    first = lax.axis_index("tm") * frame_dev - margin
    frames = first - 1 + jnp.arange(span + 2, dtype=jnp.int32)
    starts = clip_bounds[:, :clip_total]
    clip_id = jnp.sum((frames[None, :, None] >= starts[:, None, :]).astype(jnp.int32), axis=2)
    living = (frames[None, :] >= 0) & (
        frames[None, :] < clip_bounds[:, clip_total : clip_total + 1]
    )
    paired = living[:, :-1] & living[:, 1:] & (clip_id[:, :-1] == clip_id[:, 1:])
    usable = living[:, 1:-1].astype(jnp.float32)
    behind = paired[:, :span].astype(jnp.float32)
    ahead = paired[:, 1:].astype(jnp.float32)
    return (usable, (behind, jnp.ones_like(usable), ahead))


def convolve(padded, kernel, masks):
    mel_dev = padded.shape[2] - 2
    frame_dev = padded.shape[3] - 2
    result = jnp.zeros((padded.shape[0], kernel.shape[0], mel_dev, frame_dev), jnp.float32)
    for frame_step in range(3):
        partial_sum = jnp.zeros_like(result)
        for mel_step in range(3):
            piece = padded[:, :, mel_step : mel_step + mel_dev, frame_step : frame_step + frame_dev]
            partial_sum = partial_sum + jnp.einsum(
                "oc,rcmf->romf",
                kernel[:, :, mel_step, frame_step],
                piece,
                preferred_element_type=jnp.float32,
            )
        if frame_step != 1:
            partial_sum = partial_sum * masks[frame_step][:, None, None, :]
        result = result + partial_sum
    return result


def kernel_terms(grad_low, padded, masks):
    mel_dev = grad_low.shape[2]
    frame_dev = grad_low.shape[3]
    masked = [
        grad_low * masks[frame_step].astype(jnp.bfloat16)[:, None, None, :]
        for frame_step in range(3)
    ]
    table = []
    for mel_step in range(3):
        entries = []
        for frame_step in range(3):
            piece = padded[:, :, mel_step : mel_step + mel_dev, frame_step : frame_step + frame_dev]
            entries.append(
                jnp.einsum(
                    "romf,rcmf->oc", masked[frame_step], piece, preferred_element_type=jnp.float32
                )
            )
        table.append(jnp.stack(entries, axis=-1))
    return jnp.stack(table, axis=-2)


AXES = ("mel", "tm")


def gather_sum(parts, form):
    flat = jnp.concatenate([p.reshape(-1) for p in parts])
    count = lax.axis_size("mel") * lax.axis_size("tm")
    if form == "exchange":
        every = lax.all_to_all(
            jnp.broadcast_to(flat[None], (count, flat.shape[0])), AXES, 0, 0, tiled=True
        )
        total = jnp.sum(every, axis=0)
    elif form == "gather":
        total = jnp.sum(lax.all_gather(flat, AXES), axis=0)
    elif form == "two":
        total = flat
        for axis in AXES:
            every = lax.all_to_all(
                jnp.broadcast_to(total[None], (lax.axis_size(axis), flat.shape[0])),
                axis,
                0,
                0,
                tiled=True,
            )
            total = jnp.sum(every, axis=0)
    else:
        total = flat
        for axis in AXES:
            size = lax.axis_size(axis)
            step = 1
            while step < size:
                total = total + lax.ppermute(total, axis, [(i, i ^ step) for i in range(size)])
                step *= 2
    out = []
    at = 0
    for p in parts:
        out.append(total[at : at + p.size].reshape(p.shape))
        at += p.size
    return out


def scatter_gather_sum(part):
    count = lax.axis_size("mel") * lax.axis_size("tm")
    flat = part.reshape(-1)
    width = -(-flat.shape[0] // count)
    flat = jnp.pad(flat, (0, width * count - flat.shape[0])).reshape(count, width)
    mine = jnp.sum(lax.all_to_all(flat, AXES, 0, 0, tiled=True), axis=0)
    every = lax.all_gather(mine, AXES)
    return every.reshape(-1)[: part.size].reshape(part.shape)


def moments(field, usable4):
    weighted = field * usable4
    return (jnp.sum(weighted, axis=(0, 2, 3)), jnp.sum(weighted * field, axis=(0, 2, 3)))


def normalize(field, sums, pixel_count):
    average = sums[0] / pixel_count
    inv_std = lax.rsqrt(sums[1] / pixel_count - average * average + 1e-05)
    return ((field - average[None, :, None, None]) * inv_std[None, :, None, None], inv_std)


def silu_slope(scaled):
    sigma = jax.nn.sigmoid(scaled)
    return sigma * (1.0 + scaled * (1.0 - sigma))


def norm_back(grad_scaled, normed, inv_std, gain, totals, pixel_count, usable4):
    factor = (gain * inv_std)[None, :, None, None]
    centred = (
        grad_scaled
        - (totals[1][None, :, None, None] + normed * totals[0][None, :, None, None]) / pixel_count
    )
    return (factor * centred * usable4).astype(jnp.bfloat16)


def grad_halo(grad_low):
    return with_halo(grad_low, (("mel", 2), ("tm", 3)), 1)


def shards(
    spectrum,
    clip_bounds,
    kernel_one,
    gain_one,
    bias_one,
    kernel_two,
    gain_two,
    bias_two,
    pooled_grad,
):
    row_count, mel_dev, frame_dev = spectrum.shape
    chan = kernel_two.shape[0]
    usable, masks = frame_masks(clip_bounds, frame_dev, 0)
    usable4 = usable[:, None, None, :]
    pixel_count = mel_dev * lax.axis_size("mel") * jnp.sum(clip_bounds[:, -1]).astype(jnp.float32)
    masked_input = spectrum * usable.astype(jnp.bfloat16)[:, None, :]
    input_padded = with_halo(masked_input, (("mel", 1), ("tm", 2)), 1)[:, None]
    pre_one = convolve(input_padded, kernel_one[:, None], masks)
    stats_one = gather_sum(moments(pre_one, usable4), "exchange")
    normed_one, inv_one = normalize(pre_one, stats_one, pixel_count)
    scaled_one = normed_one * gain_one[None, :, None, None] + bias_one[None, :, None, None]
    act_one = (jax.nn.silu(scaled_one) * usable4).astype(jnp.bfloat16)
    act_padded = with_halo(act_one, (("mel", 2), ("tm", 3)), 1)
    pre_two = convolve(act_padded, kernel_two, masks)
    stats_two = gather_sum(moments(pre_two, usable4), "gather")
    normed_two, inv_two = normalize(pre_two, stats_two, pixel_count)
    scaled_two = normed_two * gain_two[None, :, None, None] + bias_two[None, :, None, None]
    act_two = jax.nn.silu(scaled_two) * usable4
    blocks = act_two.reshape(row_count, chan, mel_dev // 2, 2, frame_dev // 2, 2)
    pooled = jnp.mean(blocks, axis=(3, 5)).astype(jnp.bfloat16)
    upstream = pooled_grad.astype(jnp.float32)[:, :, :, None, :, None]
    upstream = (
        jnp.broadcast_to(upstream, blocks.shape).reshape(row_count, chan, mel_dev, frame_dev) * 0.25
    )
    grad_scaled_two = upstream * usable4 * silu_slope(scaled_two)
    totals_two = gather_sum(
        (
            jnp.sum(grad_scaled_two * normed_two, axis=(0, 2, 3)),
            jnp.sum(grad_scaled_two, axis=(0, 2, 3)),
        ),
        "halving",
    )
    grad_pre_two = norm_back(
        grad_scaled_two, normed_two, inv_two, gain_two, totals_two, pixel_count, usable4
    )
    kernel_two_part = kernel_terms(grad_pre_two, act_padded, masks)
    kernel_two_grad = scatter_gather_sum(kernel_two_part)
    grad_two_padded = grad_halo(grad_pre_two)
    flipped_two = jnp.transpose(jnp.flip(kernel_two, (2, 3)), (1, 0, 2, 3))
    grad_act_one = convolve(grad_two_padded, flipped_two, masks)
    grad_scaled_one = grad_act_one * usable4 * silu_slope(scaled_one)
    gain_part = jnp.sum(grad_scaled_one * normed_one, axis=(0, 2, 3))
    bias_part = jnp.sum(grad_scaled_one, axis=(0, 2, 3))
    totals_one = gather_sum((gain_part, bias_part), "two")
    grad_pre_one = norm_back(
        grad_scaled_one, normed_one, inv_one, gain_one, totals_one, pixel_count, usable4
    )
    kernel_one_part = kernel_terms(grad_pre_one, input_padded, masks)[:, 0]
    (kernel_one_grad,) = gather_sum((kernel_one_part,), "exchange")
    grad_one_padded = grad_halo(grad_pre_one)
    flipped_one = jnp.transpose(jnp.flip(kernel_one[:, None], (2, 3)), (1, 0, 2, 3))
    spectrum_grad = convolve(grad_one_padded, flipped_one, masks)[:, 0] * usable[:, None, :]
    return (
        pooled,
        spectrum_grad,
        kernel_one_grad,
        totals_one[0],
        totals_one[1],
        kernel_two_grad,
        totals_two[0],
        totals_two[1],
    )


def solution(mesh):
    return jax.shard_map(
        shards,
        mesh=mesh,
        in_specs=(
            P(None, "mel", "tm"),
            P(),
            P(),
            P(),
            P(),
            P(),
            P(),
            P(),
            P(None, None, "mel", "tm"),
        ),
        out_specs=(P(None, None, "mel", "tm"), P(None, "mel", "tm"), P(), P(), P(), P(), P(), P()),
        check_vma=False,
    )
```

```python
import jax
import jax.numpy as jnp
from jax import lax
from jax.sharding import PartitionSpec as P


def with_halo(x, sides, width):
    for axis, dim in sides:
        size, length = (lax.axis_size(axis), x.shape[dim])
        up = [(i, (i + 1) % size) for i in range(size - 1)]
        down = [(j, i) for i, j in up]
        last = lax.slice_in_dim(x, length - width, length, axis=dim)
        leading = lax.slice_in_dim(x, 0, width, axis=dim)
        before = lax.ppermute(last, axis, up)
        after = lax.ppermute(leading, axis, down)
        x = jnp.concatenate([before, x, after], axis=dim)
    return x


def frame_masks(clip_bounds, frame_dev, margin):
    clip_total = clip_bounds.shape[1] - 1
    span = frame_dev + 2 * margin
    first = lax.axis_index("tm") * frame_dev - margin
    frames = first - 1 + jnp.arange(span + 2, dtype=jnp.int32)
    starts = clip_bounds[:, :clip_total]
    clip_id = jnp.sum((frames[None, :, None] >= starts[:, None, :]).astype(jnp.int32), axis=2)
    living = (frames[None, :] >= 0) & (
        frames[None, :] < clip_bounds[:, clip_total : clip_total + 1]
    )
    paired = living[:, :-1] & living[:, 1:] & (clip_id[:, :-1] == clip_id[:, 1:])
    usable = living[:, 1:-1].astype(jnp.float32)
    behind = paired[:, :span].astype(jnp.float32)
    ahead = paired[:, 1:].astype(jnp.float32)
    return (usable, (behind, jnp.ones_like(usable), ahead))


def convolve(padded, kernel, masks):
    mel_dev = padded.shape[2] - 2
    frame_dev = padded.shape[3] - 2
    result = jnp.zeros((padded.shape[0], kernel.shape[0], mel_dev, frame_dev), jnp.float32)
    for frame_step in range(3):
        partial_sum = jnp.zeros_like(result)
        for mel_step in range(3):
            piece = padded[:, :, mel_step : mel_step + mel_dev, frame_step : frame_step + frame_dev]
            partial_sum = partial_sum + jnp.einsum(
                "oc,rcmf->romf",
                kernel[:, :, mel_step, frame_step],
                piece,
                preferred_element_type=jnp.float32,
            )
        if frame_step != 1:
            partial_sum = partial_sum * masks[frame_step][:, None, None, :]
        result = result + partial_sum
    return result


def kernel_terms(grad_low, padded, masks):
    mel_dev = grad_low.shape[2]
    frame_dev = grad_low.shape[3]
    masked = [
        grad_low * masks[frame_step].astype(jnp.bfloat16)[:, None, None, :]
        for frame_step in range(3)
    ]
    table = []
    for mel_step in range(3):
        entries = []
        for frame_step in range(3):
            piece = padded[:, :, mel_step : mel_step + mel_dev, frame_step : frame_step + frame_dev]
            entries.append(
                jnp.einsum(
                    "romf,rcmf->oc", masked[frame_step], piece, preferred_element_type=jnp.float32
                )
            )
        table.extend(entries)
    return jnp.stack(table)


AXES = ("mel", "tm")


def exchange(blocks):
    return lax.all_to_all(blocks, AXES, 0, 0, tiled=True)


def gather_sum(parts):
    flat = jnp.concatenate([p.reshape(-1) for p in parts])
    count = lax.axis_size("mel") * lax.axis_size("tm")
    total = jnp.sum(exchange(jnp.broadcast_to(flat[None], (count, flat.shape[0]))), axis=0)
    out = []
    at = 0
    for p in parts:
        out.append(total[at : at + p.size].reshape(p.shape))
        at += p.size
    return out


def scatter_gather_sum(part):
    count = lax.axis_size("mel") * lax.axis_size("tm")
    taps, outs, ins = part.shape
    share = -(-outs // count)
    part = jnp.pad(part, ((0, 0), (0, share * count - outs), (0, 0)))
    cut = jnp.transpose(part.reshape(taps, count, share, ins), (1, 0, 2, 3))
    mine = jnp.sum(exchange(cut), axis=0)
    every = exchange(jnp.broadcast_to(mine[None], (count,) + mine.shape))
    return jnp.transpose(every, (1, 0, 2, 3)).reshape(taps, count * share, ins)[:, :outs]


def moments(field, usable4):
    weighted = field * usable4
    return (jnp.sum(weighted, axis=(0, 2, 3)), jnp.sum(weighted * field, axis=(0, 2, 3)))


def normalize(field, sums, pixel_count):
    average = sums[0] / pixel_count
    inv_std = lax.rsqrt(sums[1] / pixel_count - average * average + 1e-05)
    return ((field - average[None, :, None, None]) * inv_std[None, :, None, None], inv_std)


def silu_slope(scaled):
    sigma = jax.nn.sigmoid(scaled)
    return sigma * (1.0 + scaled * (1.0 - sigma))


def norm_back(grad_scaled, normed, inv_std, gain, totals, pixel_count, usable4):
    factor = (gain * inv_std)[None, :, None, None]
    centred = (
        grad_scaled
        - (totals[1][None, :, None, None] + normed * totals[0][None, :, None, None]) / pixel_count
    )
    return (factor * centred * usable4).astype(jnp.bfloat16)


def grad_halo(grad_low):
    return with_halo(grad_low, (("mel", 2), ("tm", 3)), 1)


def shards(
    spectrum,
    clip_bounds,
    kernel_one,
    gain_one,
    bias_one,
    kernel_two,
    gain_two,
    bias_two,
    pooled_grad,
):
    row_count, mel_dev, frame_dev = spectrum.shape
    chan = kernel_two.shape[0]
    usable, masks = frame_masks(clip_bounds, frame_dev, 0)
    usable4 = usable[:, None, None, :]
    pixel_count = mel_dev * lax.axis_size("mel") * jnp.sum(clip_bounds[:, -1]).astype(jnp.float32)
    masked_input = spectrum * usable.astype(jnp.bfloat16)[:, None, :]
    input_padded = with_halo(masked_input, (("mel", 1), ("tm", 2)), 1)[:, None]
    pre_one = convolve(input_padded, kernel_one[:, None], masks)
    stats_one = gather_sum(moments(pre_one, usable4))
    normed_one, inv_one = normalize(pre_one, stats_one, pixel_count)
    scaled_one = normed_one * gain_one[None, :, None, None] + bias_one[None, :, None, None]
    act_one = (jax.nn.silu(scaled_one) * usable4).astype(jnp.bfloat16)
    act_padded = with_halo(act_one, (("mel", 2), ("tm", 3)), 1)
    pre_two = convolve(act_padded, kernel_two, masks)
    stats_two = gather_sum(moments(pre_two, usable4))
    normed_two, inv_two = normalize(pre_two, stats_two, pixel_count)
    scaled_two = normed_two * gain_two[None, :, None, None] + bias_two[None, :, None, None]
    act_two = jax.nn.silu(scaled_two) * usable4
    blocks = act_two.reshape(row_count, chan, mel_dev // 2, 2, frame_dev // 2, 2)
    pooled = jnp.mean(blocks, axis=(3, 5)).astype(jnp.bfloat16)
    upstream = pooled_grad.astype(jnp.float32)[:, :, :, None, :, None]
    upstream = (
        jnp.broadcast_to(upstream, blocks.shape).reshape(row_count, chan, mel_dev, frame_dev) * 0.25
    )
    grad_scaled_two = upstream * usable4 * silu_slope(scaled_two)
    totals_two = gather_sum(
        (
            jnp.sum(grad_scaled_two * normed_two, axis=(0, 2, 3)),
            jnp.sum(grad_scaled_two, axis=(0, 2, 3)),
        )
    )
    grad_pre_two = norm_back(
        grad_scaled_two, normed_two, inv_two, gain_two, totals_two, pixel_count, usable4
    )
    kernel_two_part = kernel_terms(grad_pre_two, act_padded, masks)
    kernel_two_grad = scatter_gather_sum(kernel_two_part)
    kernel_two_grad = jnp.transpose(kernel_two_grad.reshape(3, 3, chan, chan), (2, 3, 0, 1))
    grad_two_padded = grad_halo(grad_pre_two)
    flipped_two = jnp.transpose(jnp.flip(kernel_two, (2, 3)), (1, 0, 2, 3))
    grad_act_one = convolve(grad_two_padded, flipped_two, masks)
    grad_scaled_one = grad_act_one * usable4 * silu_slope(scaled_one)
    gain_part = jnp.sum(grad_scaled_one * normed_one, axis=(0, 2, 3))
    bias_part = jnp.sum(grad_scaled_one, axis=(0, 2, 3))
    totals_one = gather_sum((gain_part, bias_part))
    grad_pre_one = norm_back(
        grad_scaled_one, normed_one, inv_one, gain_one, totals_one, pixel_count, usable4
    )
    kernel_one_part = kernel_terms(grad_pre_one, input_padded, masks)[:, :, 0]
    (kernel_one_grad,) = gather_sum((kernel_one_part,))
    kernel_one_grad = jnp.transpose(kernel_one_grad.reshape(3, 3, chan), (2, 0, 1))
    grad_one_padded = grad_halo(grad_pre_one)
    flipped_one = jnp.transpose(jnp.flip(kernel_one[:, None], (2, 3)), (1, 0, 2, 3))
    spectrum_grad = convolve(grad_one_padded, flipped_one, masks)[:, 0] * usable[:, None, :]
    return (
        pooled,
        spectrum_grad,
        kernel_one_grad,
        totals_one[0],
        totals_one[1],
        kernel_two_grad,
        totals_two[0],
        totals_two[1],
    )


def solution(mesh):
    return jax.shard_map(
        shards,
        mesh=mesh,
        in_specs=(
            P(None, "mel", "tm"),
            P(),
            P(),
            P(),
            P(),
            P(),
            P(),
            P(),
            P(None, None, "mel", "tm"),
        ),
        out_specs=(P(None, None, "mel", "tm"), P(None, "mel", "tm"), P(), P(), P(), P(), P(), P()),
        check_vma=False,
    )
```

```python
import functools

import jax
import jax.numpy as jnp
import numpy as np
from jax import lax
from jax.experimental import pallas as pl
from jax.experimental.pallas import tpu as pltpu
from jax.sharding import PartitionSpec as P

F32 = jnp.float32
BF16 = jnp.bfloat16
AXES = ("mel", "tm")
EXACT = lax.Precision.HIGHEST
RIM = 128
BAND = 24


def iota(shape, dim):
    return lax.broadcasted_iota(jnp.int32, shape, dim)


def dot(a, b, over=((1,), (0,)), precision=None):
    return lax.dot_general(a, b, (over, ((), ())), precision=precision, preferred_element_type=F32)


def to_column(lanes, count, start=0):
    shape = (count, lanes.shape[1])
    return jnp.sum(jnp.where(iota(shape, 1) == iota(shape, 0) + start, lanes, 0.0), axis=1, keepdims=True)


def to_lanes(column, start=0, width=128):
    shape = (column.shape[0], width)
    return jnp.sum(jnp.where(iota(shape, 1) == iota(shape, 0) + start, column, 0.0), axis=0, keepdims=True)


def frame_masks(bounds, frames):
    last = bounds.shape[1] - 1

    def living(f):
        return (f >= 0) & (f < bounds[0, last])

    def paired(f):
        both = living(f) & living(f + 1)
        for k in range(1, last):
            both = both & (f + 1 != bounds[0, k])
        return both

    return tuple(m.astype(F32) for m in (living(frames), paired(frames - 1), paired(frames)))


def lane_masks(info, frame_dev):
    lane = iota((1, frame_dev + RIM), 1)
    frames = info[0, 5] * frame_dev + jnp.where(lane < frame_dev + RIM // 2, lane, lane - frame_dev - RIM)
    return frame_masks(info.at[:, 0:4], frames)


def row_valid(info, row, rows, mels):
    mel = info[0, 4] * rows + row
    return ((mel >= 0) & (mel < mels)).astype(F32)


def pixels(info, mels):
    return (info[0, 3] * mels).astype(F32)


def pack_mel(info, spec, grad, out):
    me = info[0, 4]
    x = spec[0]
    rows, frame_dev = x.shape
    half = frame_dev // 2
    g = grad[0].astype(F32)
    top = g[:, 0, :]
    bottom = g[:, g.shape[1] - 1, :]
    for j in range(out.shape[0]):
        out[j, 0:rows] = x[:, :half]
        out[j, rows : 2 * rows] = x[:, half:]
        edge = jnp.where(j == me - 1, top, 0.0) + jnp.where(j == me + 1, bottom, 0.0)
        out[j, 2 * rows :] = edge.astype(BF16)


def weights(k2, k1, select, wf, wb, w1, ws, pairs, singles, k1t):
    chan = k2.shape[1]
    span = wf.shape[1]
    rest = jnp.zeros((chan, span - 9 * chan), F32)
    taps = [k2[t].astype(F32) for t in range(9)]
    forward = jnp.concatenate(taps + [rest], axis=1)
    backward = jnp.concatenate([taps[8 - t].T for t in range(9)] + [rest], axis=1)
    for r in range(wf.shape[0] // chan):
        at = slice(r * chan, (r + 1) * chan)
        wf[at] = (pltpu.roll(forward, 3 * chan * r, 1) if r else forward).astype(BF16)
        wb[at] = (pltpu.roll(backward, 3 * chan * r, 1) if r else backward).astype(BF16)
    k1t[...] = k1[...]
    k = k1[...].astype(BF16)
    lanes = [dot(k, select[s], ((0,), (0,)))[:chan] for s in range(4)]
    pairs[...] = lanes[1] * lanes[2]
    singles[...] = lanes[3]
    for m in range(w1.shape[0] // chan):
        w1[m * chan : (m + 1) * chan] = (pltpu.roll(lanes[0], m, 1) if m else lanes[0]).astype(BF16)
    full = k1[...]
    low = [
        jnp.concatenate([full[3 * (2 - a) + 2 - b : 3 * (2 - a) + 3 - b, :chan] for a in range(3)], axis=1)
        for b in range(3)
    ]
    base = jnp.concatenate(low + [jnp.zeros((5, 3 * chan), F32)], axis=0)
    base = jnp.concatenate([base, jnp.zeros((8, span - 3 * chan), F32)], axis=1)
    for m in range(ws.shape[0] // 8):
        ws[8 * m : 8 * m + 8] = (pltpu.roll(base, chan * m, 1) if m else base).astype(BF16)


def feature_rows(shifted, axis_shift, weight):
    z = [None] * 9
    for j in range(3):
        for i in range(3):
            z[3 * i + j] = axis_shift(shifted[j], i)

    def folded(v):
        if v.shape[1] > 128:
            v = v[:, :128] + v[:, 128:]
        return jnp.sum(v, axis=0, keepdims=True)

    rows = [None] * 96
    for s in range(9):
        left = z[s] * weight
        rows[81 + s] = folded(left)
        for t in range(s, 9):
            rows[9 * s + t] = rows[9 * t + s] = folded(left * z[t])
    zero = jnp.zeros((1, 128), F32)
    stack = jnp.concatenate([zero if r is None else r for r in rows], axis=0)
    return to_lanes(jnp.sum(stack, axis=1, keepdims=True))


def pack_tm(info, recv, grad, out, spread):
    count = out.shape[0]
    n_mel = recv.shape[0]
    me_m, me_t = info[0, 4], info[0, 5]
    chan, rows = grad.shape[1], 16
    half = recv.shape[2]
    frame_dev = 2 * half
    mels = n_mel * rows
    lane = iota((1, frame_dev), 1)
    usable, behind, ahead = frame_masks(info.at[:, 0:4], me_t * frame_dev + lane)
    x = jnp.concatenate(
        [
            jnp.concatenate([recv[j, 0:rows] for j in range(n_mel)], axis=0),
            jnp.concatenate([recv[j, rows : 2 * rows] for j in range(n_mel)], axis=0),
        ],
        axis=1,
    )
    x = x.astype(F32) * usable
    inner = ((lane > 0) & (lane < frame_dev - 1)).astype(F32)
    row = iota((mels, frame_dev), 0)

    def mel_shift(v, i):
        if i == 1:
            return v
        if i == 0:
            return jnp.where(row == 0, 0.0, pltpu.roll(v, 1, 0))
        return jnp.where(row == mels - 1, 0.0, pltpu.roll(v, mels - 1, 0))

    shifted = [pltpu.roll(x, 1, 1) * behind, x, pltpu.roll(x, frame_dev - 1, 1) * ahead]
    features = feature_rows(shifted, mel_shift, inner)
    high = features.astype(BF16).astype(F32)
    mid = (features - high).astype(BF16).astype(F32)
    low = features - high - mid
    pick = iota((8, frame_dev), 0)
    column = jnp.where(pick < 4, pick, frame_dev - 8 + pick)
    edges = dot((iota((8, frame_dev), 1) == column).astype(BF16), x.astype(BF16), ((1,), (1,)))
    edges = jnp.concatenate([edges, jnp.zeros((8, 128 - mels), F32)], axis=1)
    target = iota((count, half), 0)
    at = iota((count, half), 1)
    choose = ((target == me_t - 1) & (at == 0)) | ((target == me_t + 1) & (at == half - 1))
    choose = choose.astype(BF16)
    above = recv[jnp.maximum(me_m - 1, 0), 2 * rows :]
    below = recv[jnp.minimum(me_m + 1, n_mel - 1), 2 * rows :]
    own = grad[0].astype(F32).reshape(chan * grad.shape[2], half).astype(BF16)
    columns = dot(choose, own, ((1,), (1,)))
    outer = jnp.concatenate([dot(choose, above, ((1,), (1,))), dot(choose, below, ((1,), (1,)))], axis=1)
    parts = columns.shape[1] // 128
    for q in range(parts):
        spread[pl.ds(8 + q, count, stride=16), :] = columns[:, 128 * q : 128 * (q + 1)]
    spread[pl.ds(8 + parts, count, stride=16), :] = outer
    common = jnp.concatenate([high, mid, low], axis=0)
    for j in range(count):
        tail = jnp.concatenate([spread[16 * j + 8 : 16 * j + 13, :], common], axis=0)
        out[j] = jnp.concatenate([edges, tail], axis=0).astype(BF16)


def expand(info, recv_mel, recv_tm, grad, spread, columns, out, temp):
    me_m, me_t = info[0, 4], info[0, 5]
    n_mel, count = recv_mel.shape[0], recv_tm.shape[0]
    chan, rows, half = grad.shape[1:]
    own = grad[0].astype(F32).reshape(chan * rows, half).astype(BF16)
    above = recv_mel[jnp.maximum(me_m - 1, 0), 32:]
    below = recv_mel[jnp.minimum(me_m + 1, n_mel - 1), 32:]
    every = jnp.concatenate([own, above, below], axis=0)
    after = recv_tm[jnp.minimum(me_t + 1, count - 1)].astype(F32)
    before = recv_tm[jnp.maximum(me_t - 1, 0)].astype(F32)
    after = jnp.concatenate([after[8 + q : 9 + q] for q in range(5)], axis=1)
    before = jnp.concatenate([before[8 + q : 9 + q] for q in range(5)], axis=1)
    side = iota((16, after.shape[1]), 0)
    sides = jnp.where(side == 0, after, jnp.where(side == 1, before, 0.0)).astype(BF16)
    wide = dot(every, spread[...]) + dot(sides, columns[...], ((0,), (0,)))
    for part in range(3):
        cut = slice(128 * part, 128 * (part + 1))
        temp[...] = wide[: chan * rows, cut]
        for r in range(rows):
            out[(r + 1) * chan : (r + 2) * chan, cut] = temp[pl.ds(r, chan, stride=rows), :]
    out[0:chan] = wide[chan * rows : chan * (rows + 1)]
    out[(rows + 1) * chan :] = wide[chan * (rows + 1) :]


def silu_parts(y):
    sigma = 0.5 * jnp.tanh(0.5 * y) + 0.5
    return sigma, y * sigma


def forward_one(info, recv_mel, recv_tm, place, pairs, singles, w1, wf, gain, bias,
                pre_two, payload, act, pre_one, slope, x3_out, stats, features_out, xs, x3):
    n_mel, count = recv_mel.shape[0], recv_tm.shape[0]
    rows = 16
    mels = n_mel * rows
    half = recv_mel.shape[2]
    frame_dev = 2 * half
    wide = frame_dev + RIM
    chan = gain.shape[1]
    me_m, me_t = info[0, 4], info[0, 5]
    usable, behind, ahead = lane_masks(info, frame_dev)
    total = pixels(info, mels)
    x = jnp.concatenate(
        [
            jnp.concatenate([recv_mel[j, 0:rows] for j in range(n_mel)], axis=0),
            jnp.concatenate([recv_mel[j, rows : 2 * rows] for j in range(n_mel)], axis=0),
        ],
        axis=1,
    ).astype(F32)
    after = recv_tm[jnp.minimum(me_t + 1, count - 1)].astype(F32)[0:8, :mels]
    before = recv_tm[jnp.maximum(me_t - 1, 0)].astype(F32)[0:8, :mels]
    after = jnp.where(me_t + 1 < count, after, 0.0)
    before = jnp.where(me_t > 0, before, 0.0)
    sides = jnp.concatenate([after[0:4], before[4:8], jnp.zeros((8, mels), F32)], axis=0).astype(BF16)
    x = jnp.concatenate([x, dot(sides, place[...], ((0,), (0,)))], axis=1) * usable
    xs[0:8] = jnp.zeros((8, wide), F32)
    xs[mels : mels + 8] = jnp.zeros((8, wide), F32)
    xs[4 : mels + 4] = x
    near = xs[pl.ds(pl.multiple_of(me_m * rows, 8), BAND), :]
    x3[...] = jnp.concatenate(
        [
            pltpu.roll(near, 1, 1) * behind,
            near,
            pltpu.roll(near, wide - 1, 1) * ahead,
            jnp.broadcast_to(usable, (BAND, wide)),
            jnp.zeros((128 - 4 * BAND, wide), F32),
        ],
        axis=0,
    ).astype(BF16)
    x3_out[...] = x3[:, :frame_dev]
    pre_one[...] = dot(w1[...], x3[...])
    edge = recv_tm[:, 0:8, :].astype(F32).reshape(count * 8, 128)
    place_q = iota((count * 8, 1), 0)
    k = place_q % 8
    frames = (place_q // 8) * frame_dev + jnp.where(k < 4, k, k + frame_dev - 8)
    _, q_behind, q_ahead = frame_masks(info.at[:, 0:4], frames)
    outer = ((k == 0) | (k == 7)).astype(F32)
    lane = iota((count * 8, 128), 1)

    def lane_shift(v, i):
        if i == 1:
            return v
        if i == 0:
            return jnp.where(lane < mels, pltpu.roll(v, 1, 1), 0.0)
        return pltpu.roll(v, 127, 1)

    shifted = [
        pltpu.roll(edge, 1, 0) * q_behind,
        edge,
        pltpu.roll(edge, count * 8 - 1, 0) * q_ahead,
    ]
    features = feature_rows(shifted, lane_shift, outer)
    parts = jnp.zeros((8, 128), F32)
    for d in range(count):
        parts = parts + recv_tm[d].astype(F32)[8:16]
    features = features + parts[5:6] + parts[6:7] + parts[7:8]
    features_out[...] = jnp.broadcast_to(features, (8, 128))
    mean = jnp.sum(singles[...] * features, axis=1, keepdims=True) / total
    square = jnp.sum(pairs[...] * features, axis=1, keepdims=True) / total
    inv = lax.rsqrt(square - mean * mean + 1e-05)
    lane = iota((chan, 128), 1)
    stats[0:chan] = jnp.where(lane == 0, mean, jnp.where(lane == 1, inv, 0.0))
    stats[chan : chan + 8] = jnp.broadcast_to(to_lanes(mean), (8, 128))
    stats[chan + 8 : chan + 16] = jnp.broadcast_to(to_lanes(inv), (8, 128))
    scale = to_column(gain[...], chan) * inv
    shift = to_column(bias[...], chan)
    mean = jnp.broadcast_to(mean, (chan, wide))
    scale = jnp.broadcast_to(scale, (chan, wide))
    shift = jnp.broadcast_to(shift, (chan, wide))
    ext = w1.shape[0] // chan

    def row_step(r, carry):
        at = pl.ds(pl.multiple_of(r * chan, chan), chan)
        mask = usable * row_valid(info, r - 3, rows, mels)
        y = (pre_one[at, :] - mean) * scale + shift
        sigma, value = silu_parts(y)
        slope[at, :] = sigma * (1.0 + (y - value)) * mask
        value = value * mask
        base = pl.multiple_of(r * 3 * chan, chan)
        act[pl.ds(base, chan), :] = (pltpu.roll(value, 1, 1) * behind).astype(BF16)
        act[pl.ds(base + chan, chan), :] = value.astype(BF16)
        act[pl.ds(base + 2 * chan, chan), :] = (pltpu.roll(value, wide - 1, 1) * ahead).astype(BF16)
        return carry

    lax.fori_loop(0, ext, row_step, 0)
    first = jnp.zeros((chan, frame_dev), F32)
    second = jnp.zeros((chan, frame_dev), F32)
    taps = wf.shape[1]
    for g in range(pre_two.shape[0] // wf.shape[0]):
        at = slice(g * wf.shape[0], (g + 1) * wf.shape[0])
        start = g * 3 * wf.shape[0]
        pre_two[at] = dot(wf[...], act[start : start + taps, :])

    def sum_step(q, carry):
        one, two = carry
        p = pre_two[pl.ds(pl.multiple_of(q * chan, chan), chan), :frame_dev]
        masked = p * usable[:, :frame_dev]
        return one + masked, two + masked * p

    first, second = lax.fori_loop(2, 2 + rows, sum_step, (first, second))
    first = jnp.sum(first, axis=1, keepdims=True)
    second = jnp.sum(second, axis=1, keepdims=True)
    payload[...] = jnp.broadcast_to(to_lanes(first) + to_lanes(second, chan), payload.shape)


def backward_scaled(info, recv, pre_two, up, gain, bias, grad, payload, pairs, stats):
    chan = gain.shape[1]
    rows = 16
    wide = pre_two.shape[1]
    frame_dev = wide - RIM
    mels = info[0, 6] * rows
    usable, _, _ = lane_masks(info, frame_dev)
    total = pixels(info, mels)
    sums = jnp.sum(recv[...], axis=0, keepdims=True)
    mean = to_column(sums, chan) / total
    inv = lax.rsqrt(to_column(sums, chan, chan) / total - mean * mean + 1e-05)
    lane = iota((chan, 128), 1)
    stats[...] = jnp.where(lane == 0, mean, jnp.where(lane == 1, inv, 0.0))
    mean = jnp.broadcast_to(mean, (chan, wide))
    inv = jnp.broadcast_to(inv, (chan, wide))
    scale = jnp.broadcast_to(to_column(gain[...], chan), (chan, wide))
    shift = jnp.broadcast_to(to_column(bias[...], chan), (chan, wide))

    def pair(r, carry, own):
        upstream = up[pl.ds(pl.multiple_of(r * chan, chan), chan), :]
        both = None
        for h in range(2):
            q = 2 * r + h
            at = pl.ds(pl.multiple_of(q * chan, chan), chan)
            mask = usable * row_valid(info, q - 2, rows, mels)
            normed = (pre_two[at, :] - mean) * inv
            y = normed * scale + shift
            sigma, value = silu_parts(y)
            g = upstream * (sigma * (1.0 + (y - value))) * mask
            grad[at, :] = g
            if own:
                g = g[:, :frame_dev]
                carry = (carry[0] + g * normed[:, :frame_dev], carry[1] + g)
                value = value[:, :frame_dev] * usable[:, :frame_dev]
                both = value if h == 0 else both + value
        if own:
            pairs[pl.ds(pl.multiple_of((r - 1) * chan, chan), chan), :] = both
        return carry

    zero = jnp.zeros((chan, frame_dev), F32)
    pair(0, None, False)
    last = up.shape[0] // chan - 1
    pair(last, None, False)
    first, second = lax.fori_loop(1, last, lambda r, c: pair(r, c, True), (zero, zero))
    first = jnp.sum(first, axis=1, keepdims=True)
    second = jnp.sum(second, axis=1, keepdims=True)
    payload[...] = jnp.broadcast_to(to_lanes(first) + to_lanes(second, chan), payload.shape)


def pool(pairs, mean_of, out, temp):
    chan, rows, half = out.shape[1:]
    pooled = dot(pairs[...], mean_of[...], precision=EXACT)
    for r in range(rows):
        temp[pl.ds(r, chan, stride=rows), :] = pooled[r * chan : (r + 1) * chan]
    out[0] = temp[...].reshape(chan, rows, half).astype(BF16)


def backward_two(info, recv, pre_two, grad, stats, gain, act, g3, payload, totals, own):
    chan = gain.shape[1]
    rows = 16
    wide = pre_two.shape[1]
    frame_dev = wide - RIM
    mels = info[0, 6] * rows
    usable, behind, ahead = lane_masks(info, frame_dev)
    total = pixels(info, mels)
    sums = jnp.sum(recv[...], axis=0, keepdims=True)
    totals[...] = jnp.broadcast_to(sums, (8, 128))
    mean, inv = stats[:, 0:1], stats[:, 1:2]
    factor = to_column(gain[...], chan) * inv
    gain_part = jnp.broadcast_to(to_column(sums, chan) / total * inv, (chan, wide))
    bias_part = jnp.broadcast_to(to_column(sums, chan, chan) / total, (chan, wide))
    mean = jnp.broadcast_to(mean, (chan, wide))
    factor = jnp.broadcast_to(factor, (chan, wide))
    count = pre_two.shape[0] // chan

    def row_step(q, carry):
        at = pl.ds(pl.multiple_of(q * chan, chan), chan)
        mask = usable * row_valid(info, q - 2, rows, mels)
        centred = grad[at, :] - (bias_part + (pre_two[at, :] - mean) * gain_part) * mask
        value = factor * centred
        base = pl.multiple_of(q * 3 * chan, chan)
        low = value.astype(BF16)
        g3[pl.ds(base, chan), :] = (pltpu.roll(value, 1, 1) * behind).astype(BF16)
        g3[pl.ds(base + chan, chan), :] = low
        g3[pl.ds(base + 2 * chan, chan), :] = (pltpu.roll(value, wide - 1, 1) * ahead).astype(BF16)
        own[at, :] = low[:, :frame_dev]
        return carry

    lax.fori_loop(0, count, row_step, 0)
    g3[3 * chan * count :] = jnp.zeros((6 * chan, wide), BF16)
    blank = jnp.zeros((2 * chan, frame_dev), BF16)
    own[0 : 2 * chan] = blank
    own[chan * (count - 2) :] = blank
    table = jnp.zeros((3 * chan, 3 * chan), F32)
    for m in range(rows + 2):
        left = own[m * chan : (m + 3) * chan, :]
        right = act[(m + 2) * 3 * chan : (m + 3) * 3 * chan, :frame_dev]
        table = table + dot(left, right, ((1,), (1,)))
    payload[0 : 3 * chan] = table[:, :128]
    upper = 3 * chan // 2
    payload[3 * chan :] = jnp.concatenate([table[:upper, 128:], table[upper:, 128:]], axis=1)


def backward_one(wb, g3, slope, x3, select, g1, sums):
    chan = wb.shape[0] // 4
    rows = 16
    frame_dev = x3.shape[1]
    taps = wb.shape[1]
    groups = g1.shape[0] // wb.shape[0]
    block = wb.shape[0]
    for g in range(groups):
        at = slice(g * block, (g + 1) * block)
        start = g * 3 * block
        g1[at] = dot(wb[...], g3[start : start + taps, :]) * slope[g * block + 2 * chan : (g + 1) * block + 2 * chan]
    table = jnp.zeros((chan, 128), F32)
    for g in range(rows // 4):
        part = g1[chan + g * block : chan + (g + 1) * block, :frame_dev]
        high = part.astype(BF16)
        low = (part - high.astype(F32)).astype(BF16)
        products = dot(high, x3[...], ((1,), (1,))) + dot(low, x3[...], ((1,), (1,)))
        for m in range(4):
            table = table + pltpu.roll(products[m * chan : (m + 1) * chan], 128 - (4 * g + m + 3), 1)
    rows10 = dot(select[...], table, ((1,), (1,)), EXACT)
    sums[...] = jnp.concatenate(
        [jnp.concatenate([rows10[0:5], rows10[5:10]], axis=1), jnp.zeros((3, 128), F32)], axis=0
    )


def collect(recv, sums, out):
    count = out.shape[0] // 14
    share = recv.shape[0] // count
    mine = recv[0:share, :]
    for d in range(1, count):
        mine = mine + recv[share * d : share * (d + 1), :]
    block = jnp.concatenate([sums[0:5], mine] + [jnp.zeros((9 - share, 128), F32)] * (share < 9), axis=0)
    for d in range(count):
        out[14 * d : 14 * (d + 1), :] = block


def finish(info, recv, features, stats, k1t, g1, pre_one, ws, gain, spec_grad, kernel_one, kernel_two, totals,
           low, taps_out, table):
    chan = gain.shape[1]
    rows = 16
    wide = g1.shape[1]
    frame_dev = wide - RIM
    mels = info[0, 6] * rows
    usable, behind, ahead = lane_masks(info, frame_dev)
    total = pixels(info, mels)
    count = recv.shape[0] // 14
    share = -(-9 * chan * chan // 128 // count)
    sums = recv[0:5, :]
    for d in range(1, count):
        sums = sums + recv[14 * d : 14 * d + 5, :]
    ten = jnp.concatenate([sums[:, :chan], sums[:, chan:]], axis=0)
    bias_sum = ten[9:10]
    mean_l, inv_l = stats[chan : chan + 1, :chan], stats[chan + 8 : chan + 9, :chan]
    k = k1t[0:9, :chan]
    gain_sum = inv_l * (jnp.sum(k * ten[0:9], axis=0, keepdims=True) - mean_l * bias_sum)
    totals[...] = jnp.broadcast_to(jnp.concatenate([gain_sum, bias_sum], axis=1), (8, 128))
    row = features[0:1, :]
    lane = iota((1, 128), 1)
    gram = jnp.concatenate(
        [jnp.where(lane < 9, pltpu.roll(row, 128 - 9 * t, 1) if t else row, 0.0) for t in range(9)]
        + [jnp.zeros((7, 128), F32)],
        axis=0,
    )
    single = to_column(row, 16, 81)[0:9]
    k_rows = jnp.concatenate([k1t[0:16, :chan], jnp.zeros((112, chan), F32)], axis=0)
    normed_taps = inv_l * (dot(gram, k_rows, precision=EXACT)[0:9] - single * mean_l)
    factor_l = gain[...] * inv_l
    grad_taps = factor_l * (ten[0:9] - (bias_sum * single + gain_sum * normed_taps) / total)
    kernel_one[...] = jnp.concatenate([grad_taps, jnp.zeros((7, chan), F32)], axis=0)
    mean, inv = stats[0:chan, 0:1], stats[0:chan, 1:2]
    factor = jnp.broadcast_to(to_column(gain[...], chan) * inv, (chan, wide))
    gain_part = jnp.broadcast_to(to_column(gain_sum, chan) / total * inv, (chan, wide))
    bias_part = jnp.broadcast_to(to_column(bias_sum, chan) / total, (chan, wide))
    mean = jnp.broadcast_to(mean, (chan, wide))

    def row_step(q, carry):
        at = pl.ds(pl.multiple_of(q * chan, chan), chan)
        behind_at = pl.ds(pl.multiple_of((q + 2) * chan, chan), chan)
        mask = usable * row_valid(info, q - 1, rows, mels)
        centred = g1[at, :] - (bias_part + (pre_one[behind_at, :] - mean) * gain_part) * mask
        low[at, :] = (factor * centred).astype(BF16)
        return carry

    lax.fori_loop(0, rows + 2, row_step, 0)
    taps_out[...] = dot(ws[...], low[...])
    for part in range(3):
        cut = slice(128 * part, 128 * (part + 1))
        table[part] = taps_out[:, cut]
    moved = [
        jnp.concatenate([table[part, pl.ds(b, rows, stride=8), :] for part in range(3)], axis=1) for b in range(3)
    ]
    result = pltpu.roll(moved[0], 1, 1) * behind + moved[1] + pltpu.roll(moved[2], wide - 1, 1) * ahead
    spec_grad[0] = (result * usable)[:, :frame_dev]
    whole = jnp.concatenate([recv[14 * d + 5 : 14 * d + 5 + share, :] for d in range(count)], axis=0)
    upper = 3 * chan // 2
    main = whole[: 3 * chan]
    rest = whole[3 * chan : 3 * chan + upper]
    for i in range(3):
        at = slice((2 - i) * chan, (3 - i) * chan)
        kernel_two[3 * i] = main[at, :chan]
        kernel_two[3 * i + 1] = main[at, chan:]
    last = jnp.concatenate([rest[:, :chan], rest[:, chan:]], axis=0)
    for i in range(3):
        kernel_two[3 * i + 2] = last[(2 - i) * chan : (3 - i) * chan]


def constants(frame_dev):
    half = frame_dev // 2
    select = np.zeros((4, 16, 128), np.float32)
    pick = np.zeros((16, 128), np.float32)
    for i in range(3):
        for j in range(3):
            t = 3 * i + j
            select[0, t, BAND * j + i] = 1
            pick[t, BAND * j + i] = 1
            select[1, t, 9 * t : 9 * t + 9] = 1
            select[2, t, t:81:9] = 1
            select[3, t, 81 + t] = 1
    pick[9, 3 * BAND] = 1
    spread = np.zeros((half, frame_dev + RIM), np.float32)
    spread[np.arange(frame_dev) // 2, np.arange(frame_dev)] = 0.25
    columns = np.zeros((16, frame_dev + RIM), np.float32)
    columns[0, frame_dev : frame_dev + 2] = 0.25
    columns[1, -2:] = 0.25
    place = np.zeros((16, RIM), np.float32)
    place[np.arange(4), np.arange(4)] = 1
    place[np.arange(4, 8), np.arange(4, 8) + RIM - 8] = 1
    mean_of = np.zeros((frame_dev, half), np.float32)
    mean_of[np.arange(frame_dev), np.arange(frame_dev) // 2] = 0.25
    return select, pick, spread, columns, place, mean_of


def run(kernel, outs, scratch, *args, flops=10**8, size=4 * 10**6):
    vmem = pl.BlockSpec(memory_space=pltpu.VMEM)
    return pl.pallas_call(
        kernel,
        out_shape=outs,
        in_specs=[
            pl.BlockSpec(memory_space=pltpu.SMEM) if a.dtype == jnp.int32 else vmem for a in args
        ],
        out_specs=[vmem] * len(outs),
        scratch_shapes=scratch,
        compiler_params=pltpu.CompilerParams(vmem_limit_bytes=30 * 2**20),
        cost_estimate=pl.CostEstimate(flops=flops, bytes_accessed=size, transcendentals=0),
    )(*args)


def shape(dims, dtype=F32):
    return jax.ShapeDtypeStruct(dims, dtype)


def exchange(blocks, axes=AXES):
    return lax.all_to_all(blocks, axes, 0, 0, tiled=True)


def exchange_rows(rows, axes=AXES):
    return exchange(rows[:, None, :], axes)[:, 0, :]


def shards(spectrum, clip_bounds, kernel_one, gain_one, bias_one, kernel_two, gain_two, bias_two, pooled_grad):
    _, rows, frame_dev = spectrum.shape
    chan = kernel_two.shape[0]
    n_mel, n_tm = lax.axis_size("mel"), lax.axis_size("tm")
    devices = n_mel * n_tm
    half = frame_dev // 2
    wide = frame_dev + RIM
    mels = n_mel * rows
    place_of = jnp.stack([lax.axis_index("mel"), lax.axis_index("tm"), jnp.int32(n_mel), jnp.int32(0)])
    info = jnp.concatenate([clip_bounds, place_of.astype(jnp.int32)[None]], axis=1)
    select, pick, spread, columns, place, mean_of = constants(frame_dev)
    gain_one, bias_one, gain_two, bias_two = (v[None] for v in (gain_one, bias_one, gain_two, bias_two))

    (packed,) = run(
        pack_mel, [shape((n_mel, 2 * rows + chan, half), BF16)], [], info, spectrum, pooled_grad
    )
    recv_mel = exchange(packed, "mel")
    k2 = jnp.transpose(kernel_two, (2, 3, 0, 1)).reshape(9, chan, chan)
    k1 = jnp.transpose(kernel_one, (1, 2, 0)).reshape(9, chan).astype(F32)
    k1 = jnp.pad(k1, ((0, 7), (0, 128 - chan)))
    ext = rows + 6
    span = 6 * 3 * chan
    wf, wb, w1, ws, pairs, singles, k1t = run(
        weights,
        [
            shape((4 * chan, span), BF16),
            shape((4 * chan, span), BF16),
            shape((ext * chan, 128), BF16),
            shape((rows * 8, (rows + 2) * chan), BF16),
            shape((chan, 128)),
            shape((chan, 128)),
            shape((16, 128)),
        ],
        [],
        k2,
        k1,
        jnp.asarray(select, BF16),
    )
    (packed,) = run(
        pack_tm,
        [shape((n_tm, 16, 128), BF16)],
        [pltpu.VMEM((n_tm * 16, 128), F32)],
        info,
        recv_mel,
        pooled_grad,
    )
    recv_tm = exchange(packed, "tm")
    pre_two, payload, act, pre_one, slope, x3, stats_one, features = run(
        forward_one,
        [
            shape(((rows + 4) * chan, wide)),
            shape((devices, 128)),
            shape((ext * 3 * chan, wide), BF16),
            shape((ext * chan, wide)),
            shape((ext * chan, wide)),
            shape((128, frame_dev), BF16),
            shape((chan + 16, 128)),
            shape((8, 128)),
        ],
        [pltpu.VMEM((mels + 8, wide), F32), pltpu.VMEM((128, wide), BF16)],
        info,
        recv_mel,
        recv_tm,
        jnp.asarray(place, BF16),
        pairs,
        singles,
        w1,
        wf,
        gain_one,
        bias_one,
    )
    recv = exchange_rows(payload)
    (up,) = run(
        expand,
        [shape(((rows // 2 + 2) * chan, wide))],
        [pltpu.VMEM((rows // 2 * chan, 128), F32)],
        info,
        recv_mel,
        recv_tm,
        pooled_grad,
        jnp.asarray(spread, BF16),
        jnp.asarray(columns, BF16),
    )
    grad, payload, row_pairs, stats_two = run(
        backward_scaled,
        [
            shape(((rows + 4) * chan, wide)),
            shape((devices, 128)),
            shape((rows // 2 * chan, frame_dev)),
            shape((chan, 128)),
        ],
        [],
        info,
        recv,
        pre_two,
        up,
        gain_two,
        bias_two,
    )
    recv = exchange_rows(payload)
    (pooled,) = run(
        pool,
        [shape((1, chan, rows // 2, half), BF16)],
        [pltpu.VMEM((rows // 2 * chan, 128), F32)],
        row_pairs,
        jnp.asarray(mean_of),
    )
    pieces = 9 * chan * chan // 128
    g3, payload, totals_two = run(
        backward_two,
        [shape((ext * 3 * chan, wide), BF16), shape((pieces, 128)), shape((8, 128))],
        [pltpu.VMEM(((rows + 4) * chan, frame_dev), BF16)],
        info,
        recv,
        pre_two,
        grad,
        stats_two,
        gain_two,
        act,
    )
    share = -(-pieces // devices)
    recv = exchange_rows(jnp.pad(payload, ((0, share * devices - pieces), (0, 0))))
    g1, sums = run(
        backward_one,
        [shape(((rows + 4) * chan, wide)), shape((8, 128))],
        [],
        wb,
        g3,
        slope,
        x3,
        jnp.asarray(pick),
    )
    (payload,) = run(collect, [shape((devices * 14, 128))], [], recv, sums)
    recv = exchange_rows(payload)
    spec_grad, kernel_one_grad, kernel_two_grad, totals_one = run(
        finish,
        [
            shape((1, rows, frame_dev)),
            shape((16, chan)),
            shape((9, chan, chan)),
            shape((8, 128)),
        ],
        [
            pltpu.VMEM(((rows + 2) * chan, wide), BF16),
            pltpu.VMEM((rows * 8, wide), F32),
            pltpu.VMEM((3, rows * 8, 128), F32),
        ],
        info,
        recv,
        features,
        stats_one,
        k1t,
        g1,
        pre_one,
        ws,
        gain_one,
    )
    kernel_one_grad = jnp.transpose(kernel_one_grad[:9].reshape(3, 3, chan), (2, 0, 1))
    kernel_two_grad = jnp.transpose(kernel_two_grad.reshape(3, 3, chan, chan), (2, 3, 0, 1))
    return (
        pooled,
        spec_grad,
        kernel_one_grad,
        totals_one[0, :chan],
        totals_one[0, chan:],
        kernel_two_grad,
        totals_two[0, :chan],
        totals_two[0, chan:],
    )


def solution(mesh):
    return jax.shard_map(
        shards,
        mesh=mesh,
        in_specs=(
            P(None, "mel", "tm"),
            P(),
            P(),
            P(),
            P(),
            P(),
            P(),
            P(),
            P(None, None, "mel", "tm"),
        ),
        out_specs=(P(None, None, "mel", "tm"), P(None, "mel", "tm"), P(), P(), P(), P(), P(), P()),
        check_vma=False,
    )
```

```python
import functools

import jax
import jax.numpy as jnp
from jax import lax
from jax.experimental import pallas as pl
from jax.experimental.pallas import tpu as pltpu
from jax.sharding import PartitionSpec as P

F32 = jnp.float32
BF16 = jnp.bfloat16
AXES = ("mel", "tm")
EXACT = lax.Precision.HIGHEST
RIM = 128
BAND = 24
MEL_ROWS = 16


def iota(shape, dim):
    return lax.broadcasted_iota(jnp.int32, shape, dim)


def dot(a, b, over=((1,), (0,)), precision=None):
    return lax.dot_general(a, b, (over, ((), ())), precision=precision, preferred_element_type=F32)


def to_column(lanes, count, start=0):
    shape = (count, lanes.shape[1])
    return jnp.sum(jnp.where(iota(shape, 1) == iota(shape, 0) + start, lanes, 0.0), axis=1, keepdims=True)


def to_lanes(column, start=0, width=128):
    shape = (column.shape[0], width)
    return jnp.sum(jnp.where(iota(shape, 1) == iota(shape, 0) + start, column, 0.0), axis=0, keepdims=True)


def frame_masks(bounds, frames):
    last = bounds.shape[1] - 1

    def living(f):
        return (f >= 0) & (f < bounds[0, last])

    def paired(f):
        both = living(f) & living(f + 1)
        for k in range(1, last):
            both = both & (f + 1 != bounds[0, k])
        return both

    return tuple(m.astype(F32) for m in (living(frames), paired(frames - 1), paired(frames)))


def row_valid(row, rows):
    mel = lax.axis_index("mel") * rows + row
    return ((mel >= 0) & (mel < lax.axis_size("mel") * rows)).astype(F32)


def load_all(*pairs, sems):
    copies = [pltpu.make_async_copy(src, dst, sems.at[n]) for n, (src, dst) in enumerate(pairs)]
    for copy in copies:
        copy.start()
    for copy in copies:
        copy.wait()


def pack_mel(spec_hbm, grad_hbm, out, own, spec, grad, sems):
    load_all((spec_hbm, spec), (grad_hbm, grad), sems=sems)
    me = lax.axis_index("mel")
    x = spec[0]
    rows, frame_dev = x.shape
    half = frame_dev // 2
    g = grad[0].astype(F32)
    top = g[:, 0, :]
    bottom = g[:, g.shape[1] - 1, :]
    for j in range(out.shape[0]):
        out[j, 0:rows] = x[:, :half]
        out[j, rows : 2 * rows] = x[:, half:]
        edge = jnp.where(j == me - 1, top, 0.0) + jnp.where(j == me + 1, bottom, 0.0)
        out[j, 2 * rows :] = edge.astype(BF16)
    own[...] = g.reshape(own.shape).astype(BF16)


def weights(bounds, k2_hbm, k1_hbm, gain_one_hbm, bias_one_hbm, gain_two_hbm, bias_two_hbm,
            wf, wb, w1, ws, pairs, singles, k1t, params, masks, edge_masks, twice, k2, k1, vectors, sems):
    load_all(
        (k2_hbm, k2),
        (k1_hbm, k1),
        (gain_one_hbm, vectors.at[0]),
        (bias_one_hbm, vectors.at[1]),
        (gain_two_hbm, vectors.at[2]),
        (bias_two_hbm, vectors.at[3]),
        sems=sems,
    )
    chan = k2.shape[1]
    span = wf.shape[1]
    wide = masks.shape[1]
    frame_dev = wide - RIM
    lane = iota((1, wide), 1)
    frames = lax.axis_index("tm") * frame_dev + jnp.where(lane < frame_dev + RIM // 2, lane, lane - wide)
    last = bounds.shape[1] - 1
    pixels = (bounds[0, last] * (lax.axis_size("mel") * MEL_ROWS)).astype(F32)
    masks[...] = jnp.concatenate(
        list(frame_masks(bounds, frames)) + [jnp.full((1, wide), 1.0) * pixels, jnp.zeros((4, wide), F32)], axis=0
    )
    q = iota(edge_masks.shape, 0)
    lane = iota(edge_masks.shape, 1)
    k = q % 8
    frames = (q // 8) * frame_dev + jnp.where(k < 4, k, k + frame_dev - 8)
    living, behind, ahead = frame_masks(bounds, frames)
    living = jnp.where((k == 0) | (k == 7), living, 0.0)
    edge_masks[...] = jnp.where(lane == 0, living, jnp.where(lane == 1, behind, jnp.where(lane == 2, ahead, 0.0)))
    params[...] = jnp.concatenate(
        [vectors[n] for n in range(4)] + [jnp.zeros((4, chan), F32)], axis=0
    )
    tap = iota((16, 128), 0)
    lane = iota((16, 128), 1)
    i = (tap * 11) >> 5
    ninth = (lane * 57) >> 9
    to_band = (lane == BAND * (tap - 3 * i) + i) & (tap < 9)
    to_left = (ninth == tap) & (tap < 9)
    to_right = (lane - 9 * ninth == tap) & (lane < 81)
    to_single = (lane == 81 + tap) & (tap < 9)
    source = iota((128, 128), 0) - 81
    lane = iota((128, 128), 1)
    ninth = (lane * 57) >> 9
    inside = (source >= 0) & (source < 9) & (lane < 81)
    twice[...] = jnp.where(inside, (source == ninth).astype(F32) + (source == lane - 9 * ninth).astype(F32), 0.0)
    taps = [k2[t].astype(F32) for t in range(9)]
    rest = jnp.zeros((chan, span - 9 * chan), F32)
    forward = jnp.concatenate(taps + [rest], axis=1)
    backward = jnp.concatenate([taps[8 - t].T for t in range(9)] + [rest], axis=1)
    for r in range(wf.shape[0] // chan):
        at = slice(r * chan, (r + 1) * chan)
        wf[at] = (pltpu.roll(forward, 3 * chan * r, 1) if r else forward).astype(BF16)
        wb[at] = (pltpu.roll(backward, 3 * chan * r, 1) if r else backward).astype(BF16)
    full = jnp.concatenate([k1[n].astype(F32) for n in range(3)] + [jnp.zeros((7, chan), F32)], axis=0)
    k1t[...] = full
    k = full.astype(BF16)
    lanes = [dot(k, select.astype(BF16), ((0,), (0,))) for select in (to_band, to_left, to_right, to_single)]
    pairs[...] = lanes[1] * lanes[2]
    singles[...] = lanes[3]
    for m in range(w1.shape[0] // chan):
        w1[m * chan : (m + 1) * chan] = (pltpu.roll(lanes[0], m, 1) if m else lanes[0]).astype(BF16)
    low = [
        jnp.concatenate([full[3 * (2 - a) + 2 - b : 3 * (2 - a) + 3 - b] for a in range(3)], axis=1)
        for b in range(3)
    ]
    base = jnp.concatenate(low + [jnp.zeros((5, 3 * chan), F32)], axis=0)
    base = jnp.concatenate([base, jnp.zeros((8, ws.shape[1] - 3 * chan), F32)], axis=1)
    for m in range(ws.shape[0] // 8):
        ws[8 * m : 8 * m + 8] = (pltpu.roll(base, chan * m, 1) if m else base).astype(BF16)


def feature_rows(shifted, axis_shift, weight, centre):
    z = [None] * 9
    for j in range(3):
        for i in range(3):
            z[3 * i + j] = axis_shift(shifted[j], i) - centre

    def folded(v):
        if v.shape[1] > 128:
            v = v[:, :128] + v[:, 128:]
        return jnp.sum(v, axis=0, keepdims=True)

    rows = [None] * 96
    for s in range(9):
        left = z[s] * weight
        rows[81 + s] = folded(left)
        for t in range(s, 9):
            rows[9 * s + t] = rows[9 * t + s] = folded(left * z[t])
    zero = jnp.zeros((1, 128), F32)
    stack = jnp.concatenate([zero if r is None else r for r in rows], axis=0)
    return to_lanes(jnp.sum(stack, axis=1, keepdims=True))


def pack_tm(recv, own, masks, out, spread):
    count = out.shape[0]
    n_mel = recv.shape[0]
    me_m, me_t = lax.axis_index("mel"), lax.axis_index("tm")
    rows = MEL_ROWS
    half = recv.shape[2]
    frame_dev = 2 * half
    mels = n_mel * rows
    lane = iota((1, frame_dev), 1)
    usable, behind, ahead = (masks[n : n + 1, :frame_dev] for n in range(3))
    x = jnp.concatenate(
        [
            jnp.concatenate([recv[j, 0:rows] for j in range(n_mel)], axis=0),
            jnp.concatenate([recv[j, rows : 2 * rows] for j in range(n_mel)], axis=0),
        ],
        axis=1,
    )
    x = x.astype(F32) * usable
    inner = jnp.where((lane > 0) & (lane < frame_dev - 1), usable, 0.0)
    number = mels * jnp.sum(inner, axis=1, keepdims=True)
    centre = jnp.sum(jnp.sum(x, axis=0, keepdims=True), axis=1, keepdims=True)
    centre = centre / (mels * jnp.maximum(jnp.sum(usable, axis=1, keepdims=True), 1.0))
    centre = lax.reduce_precision(centre, 8, 7)
    row = iota((mels, frame_dev), 0)

    def mel_shift(v, i):
        if i == 1:
            return v
        if i == 0:
            return jnp.where(row == 0, 0.0, pltpu.roll(v, 1, 0))
        return jnp.where(row == mels - 1, 0.0, pltpu.roll(v, mels - 1, 0))

    shifted = [pltpu.roll(x, 1, 1) * behind, x, pltpu.roll(x, frame_dev - 1, 1) * ahead]
    features = feature_rows(shifted, mel_shift, inner, centre)
    lane = iota((1, 128), 1)
    features = jnp.where(lane == 90, centre, jnp.where(lane == 91, number, features))
    high = lax.reduce_precision(features, 8, 7)
    mid = lax.reduce_precision(features - high, 8, 7)
    low = features - high - mid
    pick = iota((8, frame_dev), 0)
    column = jnp.where(pick < 4, pick, frame_dev - 8 + pick)
    edges = dot((iota((8, frame_dev), 1) == column).astype(BF16), x.astype(BF16), ((1,), (1,)))
    edges = jnp.concatenate([edges, jnp.zeros((8, 128 - mels), F32)], axis=1)
    target = iota((count, half), 0)
    at = iota((count, half), 1)
    choose = ((target == me_t - 1) & (at == 0)) | ((target == me_t + 1) & (at == half - 1))
    choose = choose.astype(BF16)
    above = recv[jnp.maximum(me_m - 1, 0), 2 * rows :]
    below = recv[jnp.minimum(me_m + 1, n_mel - 1), 2 * rows :]
    columns = dot(choose, own[...], ((1,), (1,)))
    outer = jnp.concatenate([dot(choose, above, ((1,), (1,))), dot(choose, below, ((1,), (1,)))], axis=1)
    parts = columns.shape[1] // 128
    for q in range(parts):
        spread[pl.ds(8 + q, count, stride=16), :] = columns[:, 128 * q : 128 * (q + 1)]
    spread[pl.ds(8 + parts, count, stride=16), :] = outer
    common = jnp.concatenate([high, mid, low], axis=0)
    for j in range(count):
        tail = jnp.concatenate([spread[16 * j + 8 : 16 * j + 13, :], common], axis=0)
        out[j] = jnp.concatenate([edges, tail], axis=0).astype(BF16)


def expand(recv_mel, recv_tm, own, out, temp):
    me_m, me_t = lax.axis_index("mel"), lax.axis_index("tm")
    n_mel, count = recv_mel.shape[0], recv_tm.shape[0]
    half = own.shape[1]
    rows = MEL_ROWS // 2
    chan = own.shape[0] // rows
    wide = out.shape[1]
    above = recv_mel[jnp.maximum(me_m - 1, 0), 2 * MEL_ROWS :]
    below = recv_mel[jnp.minimum(me_m + 1, n_mel - 1), 2 * MEL_ROWS :]
    every = jnp.concatenate([own[...], above, below], axis=0)
    after = recv_tm[jnp.minimum(me_t + 1, count - 1)].astype(F32)
    before = recv_tm[jnp.maximum(me_t - 1, 0)].astype(F32)
    after = jnp.concatenate([after[8 + q : 9 + q] for q in range(5)], axis=1)
    before = jnp.concatenate([before[8 + q : 9 + q] for q in range(5)], axis=1)
    side = iota((16, after.shape[1]), 0)
    sides = jnp.where(side == 0, after, jnp.where(side == 1, before, 0.0)).astype(BF16)
    lane = iota((half, wide), 1)
    spread = jnp.where((lane >> 1 == iota((half, wide), 0)) & (lane < 2 * half), 0.25, 0.0).astype(BF16)
    lane = iota((16, wide), 1)
    side = iota((16, wide), 0)
    right = (side == 0) & (lane >= 2 * half) & (lane < 2 * half + 2)
    left = (side == 1) & (lane >= wide - 2)
    columns = jnp.where(right | left, 0.25, 0.0).astype(BF16)
    full = dot(every, spread) + dot(sides, columns, ((0,), (0,)))
    for part in range(wide // 128):
        cut = slice(128 * part, 128 * (part + 1))
        temp[...] = full[: chan * rows, cut]
        for r in range(rows):
            out[(r + 1) * chan : (r + 2) * chan, cut] = temp[pl.ds(r, chan, stride=rows), :]
    out[0:chan] = full[chan * rows : chan * (rows + 1)]
    out[(rows + 1) * chan :] = full[chan * (rows + 1) :]


def silu_parts(y):
    sigma = 0.5 * jnp.tanh(0.5 * y) + 0.5
    return sigma, y * sigma


def forward_one(recv_mel, recv_tm, pairs, singles, twice, w1, wf, params, masks, edge_masks,
                pre_two, payload, act, pre_one, slope, x3, stats, features_out, xs):
    n_mel, count = recv_mel.shape[0], recv_tm.shape[0]
    rows = MEL_ROWS
    mels = n_mel * rows
    half = recv_mel.shape[2]
    frame_dev = 2 * half
    wide = frame_dev + RIM
    chan = params.shape[1]
    me_m, me_t = lax.axis_index("mel"), lax.axis_index("tm")
    usable, behind, ahead = (masks[n : n + 1] for n in range(3))
    total = masks[3:4, 0:1]
    x = jnp.concatenate(
        [
            jnp.concatenate([recv_mel[j, 0:rows] for j in range(n_mel)], axis=0),
            jnp.concatenate([recv_mel[j, rows : 2 * rows] for j in range(n_mel)], axis=0),
        ],
        axis=1,
    ).astype(F32)
    after = recv_tm[jnp.minimum(me_t + 1, count - 1)].astype(F32)[0:8, :mels]
    before = recv_tm[jnp.maximum(me_t - 1, 0)].astype(F32)[0:8, :mels]
    after = jnp.where(me_t + 1 < count, after, 0.0)
    before = jnp.where(me_t > 0, before, 0.0)
    sides = jnp.concatenate([after[0:4], before[4:8], jnp.zeros((8, mels), F32)], axis=0).astype(BF16)
    side = iota((16, RIM), 0)
    place = iota((16, RIM), 1) == jnp.where(side < 4, side, jnp.where(side < 8, side + RIM - 8, -1))
    x = jnp.concatenate([x, dot(sides, place.astype(BF16), ((0,), (0,)))], axis=1) * usable
    xs[0:8] = jnp.zeros((8, wide), F32)
    xs[mels : mels + 8] = jnp.zeros((8, wide), F32)
    xs[4 : mels + 4] = x
    near = xs[pl.ds(pl.multiple_of(me_m * rows, 8), BAND), :]
    x3[...] = jnp.concatenate(
        [
            pltpu.roll(near, 1, 1) * behind,
            near,
            pltpu.roll(near, wide - 1, 1) * ahead,
            jnp.broadcast_to(usable, (BAND, wide)),
            jnp.zeros((128 - 4 * BAND, wide), F32),
        ],
        axis=0,
    ).astype(BF16)
    pre_one[...] = dot(w1[...], x3[...])
    parts = [recv_tm[d].astype(F32)[8:16] for d in range(count)]
    parts = [p[5:6] + p[6:7] + p[7:8] for p in parts]
    centres = [p[:, 90:91] for p in parts]
    numbers = [p[:, 91:92] for p in parts]
    weight = functools.reduce(jnp.add, numbers)
    centre = functools.reduce(jnp.add, [c * n for c, n in zip(centres, numbers)]) / jnp.maximum(weight, 1.0)
    lane = iota((1, 128), 1)
    features = jnp.zeros((1, 128), F32)
    moved = jnp.zeros((1, 128), F32)
    for part, c, n in zip(parts, centres, numbers):
        delta = c - centre
        moved = moved + delta * part
        features = features + part + delta * n * jnp.where(lane < 81, delta, 1.0)
    moved = dot(jnp.broadcast_to(moved, (8, 128)), twice[...], precision=EXACT)[0:1]
    features = features + moved
    edge = recv_tm[:, 0:8, :].astype(F32).reshape(count * 8, 128)
    q_usable, q_behind, q_ahead = (edge_masks[:, n : n + 1] for n in range(3))
    lane = iota((count * 8, 128), 1)

    def lane_shift(v, i):
        if i == 1:
            return v
        if i == 0:
            return jnp.where(lane < mels, pltpu.roll(v, 1, 1), 0.0)
        return pltpu.roll(v, 127, 1)

    shifted = [
        pltpu.roll(edge, 1, 0) * q_behind,
        edge,
        pltpu.roll(edge, count * 8 - 1, 0) * q_ahead,
    ]
    features = features + feature_rows(shifted, lane_shift, jnp.where(lane < mels, q_usable, 0.0), centre)
    features = jnp.where(iota((1, 128), 1) < 90, features, 0.0)
    features_out[...] = jnp.concatenate(
        [features, jnp.broadcast_to(centre, (1, 128)), jnp.zeros((6, 128), F32)], axis=0
    )
    near_mean = jnp.sum(singles[...] * features, axis=1, keepdims=True) / total
    square = jnp.sum(pairs[...] * features, axis=1, keepdims=True) / total
    inv = lax.rsqrt(square - near_mean * near_mean + 1e-05)
    mean = near_mean + centre * jnp.sum(singles[...], axis=1, keepdims=True)
    lane = iota((chan, 128), 1)
    stats[0:chan] = jnp.where(lane == 0, mean, jnp.where(lane == 1, inv, 0.0))
    stats[chan : chan + 8] = jnp.broadcast_to(to_lanes(near_mean), (8, 128))
    stats[chan + 8 : chan + 16] = jnp.broadcast_to(to_lanes(inv), (8, 128))
    scale = to_column(params[0:1], chan) * inv
    shift = to_column(params[1:2], chan)
    mean = jnp.broadcast_to(mean, (chan, wide))
    scale = jnp.broadcast_to(scale, (chan, wide))
    shift = jnp.broadcast_to(shift, (chan, wide))
    ext = w1.shape[0] // chan

    def row_step(r, carry):
        at = pl.ds(pl.multiple_of(r * chan, chan), chan)
        mask = usable * row_valid(r - 3, rows)
        y = (pre_one[at, :] - mean) * scale + shift
        sigma, value = silu_parts(y)
        slope[at, :] = sigma * (1.0 + (y - value)) * mask
        value = value * mask
        base = pl.multiple_of(r * 3 * chan, chan)
        act[pl.ds(base, chan), :] = (pltpu.roll(value, 1, 1) * behind).astype(BF16)
        act[pl.ds(base + chan, chan), :] = value.astype(BF16)
        act[pl.ds(base + 2 * chan, chan), :] = (pltpu.roll(value, wide - 1, 1) * ahead).astype(BF16)
        return carry

    lax.fori_loop(0, ext, row_step, 0)
    first = jnp.zeros((chan, frame_dev), F32)
    second = jnp.zeros((chan, frame_dev), F32)
    taps = wf.shape[1]
    for g in range(pre_two.shape[0] // wf.shape[0]):
        at = slice(g * wf.shape[0], (g + 1) * wf.shape[0])
        start = g * 3 * wf.shape[0]
        pre_two[at] = dot(wf[...], act[start : start + taps, :])

    def sum_step(q, carry):
        one, two = carry
        p = pre_two[pl.ds(pl.multiple_of(q * chan, chan), chan), :frame_dev]
        masked = p * usable[:, :frame_dev]
        return one + masked, two + masked * p

    first, second = lax.fori_loop(2, 2 + rows, sum_step, (first, second))
    first = jnp.sum(first, axis=1, keepdims=True)
    second = jnp.sum(second, axis=1, keepdims=True)
    payload[...] = jnp.broadcast_to(to_lanes(first) + to_lanes(second, chan), payload.shape)


def backward_scaled(recv, pre_two, up, params, masks, grad, payload, pairs, stats):
    chan = params.shape[1]
    rows = MEL_ROWS
    wide = pre_two.shape[1]
    frame_dev = wide - RIM
    usable = masks[0:1]
    total = masks[3:4, 0:1]
    sums = jnp.sum(recv[...], axis=0, keepdims=True)
    mean = to_column(sums, chan) / total
    inv = lax.rsqrt(to_column(sums, chan, chan) / total - mean * mean + 1e-05)
    lane = iota((chan, 128), 1)
    stats[...] = jnp.where(lane == 0, mean, jnp.where(lane == 1, inv, 0.0))
    mean = jnp.broadcast_to(mean, (chan, wide))
    inv = jnp.broadcast_to(inv, (chan, wide))
    scale = jnp.broadcast_to(to_column(params[2:3], chan), (chan, wide))
    shift = jnp.broadcast_to(to_column(params[3:4], chan), (chan, wide))

    def pair(r, carry, own):
        upstream = up[pl.ds(pl.multiple_of(r * chan, chan), chan), :]
        both = None
        for h in range(2):
            q = 2 * r + h
            at = pl.ds(pl.multiple_of(q * chan, chan), chan)
            mask = usable * row_valid(q - 2, rows)
            normed = (pre_two[at, :] - mean) * inv
            y = normed * scale + shift
            sigma, value = silu_parts(y)
            g = upstream * (sigma * (1.0 + (y - value))) * mask
            grad[at, :] = g
            if own:
                g = g[:, :frame_dev]
                carry = (carry[0] + g * normed[:, :frame_dev], carry[1] + g)
                value = value[:, :frame_dev] * usable[:, :frame_dev]
                both = value if h == 0 else both + value
        if own:
            pairs[pl.ds(pl.multiple_of((r - 1) * chan, chan), chan), :] = both
        return carry

    zero = jnp.zeros((chan, frame_dev), F32)
    pair(0, None, False)
    last = up.shape[0] // chan - 1
    pair(last, None, False)
    first, second = lax.fori_loop(1, last, lambda r, c: pair(r, c, True), (zero, zero))
    first = jnp.sum(first, axis=1, keepdims=True)
    second = jnp.sum(second, axis=1, keepdims=True)
    payload[...] = jnp.broadcast_to(to_lanes(first) + to_lanes(second, chan), payload.shape)


def pool(pairs, out, temp):
    chan, rows, half = out.shape[1:]
    to_mean = jnp.where(iota((2 * half, half), 0) >> 1 == iota((2 * half, half), 1), 0.25, 0.0)
    pooled = dot(pairs[...], to_mean, precision=EXACT)
    for r in range(rows):
        temp[pl.ds(r, chan, stride=rows), :] = pooled[r * chan : (r + 1) * chan]
    out[0] = temp[...].reshape(chan, rows, half).astype(BF16)


def backward_two(recv, pre_two, grad, stats, params, masks, act, g3, payload, gain_out, bias_out, own):
    chan = params.shape[1]
    rows = MEL_ROWS
    wide = pre_two.shape[1]
    frame_dev = wide - RIM
    usable, behind, ahead = (masks[n : n + 1] for n in range(3))
    total = masks[3:4, 0:1]
    sums = jnp.sum(recv[...], axis=0, keepdims=True)
    gain_out[...] = sums[:, :chan]
    bias_out[...] = sums[:, chan:]
    mean, inv = stats[:, 0:1], stats[:, 1:2]
    factor = to_column(params[2:3], chan) * inv
    gain_part = jnp.broadcast_to(to_column(sums, chan) / total * inv, (chan, wide))
    bias_part = jnp.broadcast_to(to_column(sums, chan, chan) / total, (chan, wide))
    mean = jnp.broadcast_to(mean, (chan, wide))
    factor = jnp.broadcast_to(factor, (chan, wide))
    count = pre_two.shape[0] // chan

    def row_step(q, carry):
        at = pl.ds(pl.multiple_of(q * chan, chan), chan)
        mask = usable * row_valid(q - 2, rows)
        centred = grad[at, :] - (bias_part + (pre_two[at, :] - mean) * gain_part) * mask
        value = factor * centred
        base = pl.multiple_of(q * 3 * chan, chan)
        low = value.astype(BF16)
        g3[pl.ds(base, chan), :] = (pltpu.roll(value, 1, 1) * behind).astype(BF16)
        g3[pl.ds(base + chan, chan), :] = low
        g3[pl.ds(base + 2 * chan, chan), :] = (pltpu.roll(value, wide - 1, 1) * ahead).astype(BF16)
        own[at, :] = low[:, :frame_dev]
        return carry

    lax.fori_loop(0, count, row_step, 0)
    g3[3 * chan * count :] = jnp.zeros((6 * chan, wide), BF16)
    blank = jnp.zeros((2 * chan, frame_dev), BF16)
    own[0 : 2 * chan] = blank
    own[chan * (count - 2) :] = blank
    table = jnp.zeros((3 * chan, 3 * chan), F32)
    for m in range(rows + 2):
        left = own[m * chan : (m + 3) * chan, :]
        right = act[(m + 2) * 3 * chan : (m + 3) * 3 * chan, :frame_dev]
        table = table + dot(left, right, ((1,), (1,)))
    payload[0 : 3 * chan] = table[:, :128]
    upper = 3 * chan // 2
    payload[3 * chan :] = jnp.concatenate([table[:upper, 128:], table[upper:, 128:]], axis=1)


def backward_one(wb, g3, slope, x3, g1, sums):
    chan = wb.shape[0] // 4
    rows = MEL_ROWS
    frame_dev = x3.shape[1] - RIM
    taps = wb.shape[1]
    groups = g1.shape[0] // wb.shape[0]
    block = wb.shape[0]
    for g in range(groups):
        at = slice(g * block, (g + 1) * block)
        start = g * 3 * block
        g1[at] = dot(wb[...], g3[start : start + taps, :]) * slope[g * block + 2 * chan : (g + 1) * block + 2 * chan]
    table = jnp.zeros((chan, 128), F32)
    for g in range(rows // 4):
        part = g1[chan + g * block : chan + (g + 1) * block, :frame_dev]
        high = lax.reduce_precision(part, 8, 7)
        low = (part - high).astype(BF16)
        taps_in = x3[:, :frame_dev]
        products = dot(high.astype(BF16), taps_in, ((1,), (1,))) + dot(low, taps_in, ((1,), (1,)))
        for m in range(4):
            table = table + pltpu.roll(products[m * chan : (m + 1) * chan], 128 - (4 * g + m + 3), 1)
    tap = iota((16, 128), 0)
    lane = iota((16, 128), 1)
    i = (tap * 11) >> 5
    select = ((lane == BAND * (tap - 3 * i) + i) & (tap < 9)) | ((lane == 3 * BAND) & (tap == 9))
    rows10 = dot(select.astype(F32), table, ((1,), (1,)), EXACT)
    sums[...] = jnp.concatenate(
        [jnp.concatenate([rows10[0:5], rows10[5:10]], axis=1), jnp.zeros((3, 128), F32)], axis=0
    )


def collect(recv, sums, out):
    count = out.shape[0] // 14
    share = recv.shape[0] // count
    mine = recv[0:share, :]
    for d in range(1, count):
        mine = mine + recv[share * d : share * (d + 1), :]
    block = jnp.concatenate([sums[0:5], mine] + [jnp.zeros((9 - share, 128), F32)] * (share < 9), axis=0)
    for d in range(count):
        out[14 * d : 14 * (d + 1), :] = block


def finish(recv, features, stats, k1t, g1, pre_one, ws, params, masks,
           spec_grad, kernel_one, kernel_two, gain_out, bias_out, low, taps_out, table):
    chan = params.shape[1]
    rows = MEL_ROWS
    wide = g1.shape[1]
    frame_dev = wide - RIM
    usable, behind, ahead = (masks[n : n + 1] for n in range(3))
    total = masks[3:4, 0:1]
    gain = params[0:1]
    count = recv.shape[0] // 14
    share = -(-9 * chan * chan // 128 // count)
    sums = recv[0:5, :]
    for d in range(1, count):
        sums = sums + recv[14 * d : 14 * d + 5, :]
    ten = jnp.concatenate([sums[:, :chan], sums[:, chan:]], axis=0)
    bias_sum = ten[9:10]
    mean_l, inv_l = stats[chan : chan + 1, :chan], stats[chan + 8 : chan + 9, :chan]
    ten = ten - features[1:2, 0:1] * bias_sum
    k = k1t[0:9]
    gain_sum = inv_l * (jnp.sum(k * ten[0:9], axis=0, keepdims=True) - mean_l * bias_sum)
    gain_out[...] = gain_sum
    bias_out[...] = bias_sum
    row = features[0:1, :]
    lane = iota((1, 128), 1)
    gram = jnp.concatenate(
        [jnp.where(lane < 9, pltpu.roll(row, 128 - 9 * t, 1) if t else row, 0.0) for t in range(9)]
        + [jnp.zeros((7, 128), F32)],
        axis=0,
    )
    single = to_column(row, 16, 81)[0:9]
    k_rows = jnp.concatenate([k1t[...], jnp.zeros((112, chan), F32)], axis=0)
    normed_taps = inv_l * (dot(gram, k_rows, precision=EXACT)[0:9] - single * mean_l)
    factor_l = gain * inv_l
    grad_taps = factor_l * (ten[0:9] - (bias_sum * single + gain_sum * normed_taps) / total)
    for i in range(3):
        kernel_one[i] = grad_taps[3 * i : 3 * i + 3]
    mean, inv = stats[0:chan, 0:1], stats[0:chan, 1:2]
    factor = jnp.broadcast_to(to_column(gain, chan) * inv, (chan, wide))
    gain_part = jnp.broadcast_to(to_column(gain_sum, chan) / total * inv, (chan, wide))
    bias_part = jnp.broadcast_to(to_column(bias_sum, chan) / total, (chan, wide))
    mean = jnp.broadcast_to(mean, (chan, wide))

    def row_step(q, carry):
        at = pl.ds(pl.multiple_of(q * chan, chan), chan)
        behind_at = pl.ds(pl.multiple_of((q + 2) * chan, chan), chan)
        mask = usable * row_valid(q - 1, rows)
        centred = g1[at, :] - (bias_part + (pre_one[behind_at, :] - mean) * gain_part) * mask
        low[at, :] = (factor * centred).astype(BF16)
        return carry

    lax.fori_loop(0, rows + 2, row_step, 0)
    taps_out[...] = dot(ws[...], low[...])
    for part in range(3):
        cut = slice(128 * part, 128 * (part + 1))
        table[part] = taps_out[:, cut]
    moved = [
        jnp.concatenate([table[part, pl.ds(b, rows, stride=8), :] for part in range(3)], axis=1) for b in range(3)
    ]
    result = pltpu.roll(moved[0], 1, 1) * behind + moved[1] + pltpu.roll(moved[2], wide - 1, 1) * ahead
    spec_grad[0] = (result * usable)[:, :frame_dev]
    whole = jnp.concatenate([recv[14 * d + 5 : 14 * d + 5 + share, :] for d in range(count)], axis=0)
    upper = 3 * chan // 2
    main = whole[: 3 * chan]
    rest = whole[3 * chan : 3 * chan + upper]
    for i in range(3):
        at = slice((2 - i) * chan, (3 - i) * chan)
        kernel_two[3 * i] = main[at, :chan]
        kernel_two[3 * i + 1] = main[at, chan:]
    last = jnp.concatenate([rest[:, :chan], rest[:, chan:]], axis=0)
    for i in range(3):
        kernel_two[3 * i + 2] = last[(2 - i) * chan : (3 - i) * chan]


def run(kernel, outs, scratch, *args, hbm=0, flops=10**8, size=4 * 10**6):
    vmem = pl.BlockSpec(memory_space=pltpu.VMEM)
    specs = []
    args = list(args)
    for n, a in enumerate(args):
        if a.dtype == jnp.int32:
            specs.append(pl.BlockSpec(memory_space=pltpu.SMEM))
        elif hbm and n >= len(args) - hbm:
            specs.append(pl.BlockSpec(memory_space=pltpu.HBM))
            args[n] = pltpu.with_memory_space_constraint(a, pltpu.HBM)
        else:
            specs.append(vmem)
            args[n] = pltpu.with_memory_space_constraint(a, pltpu.VMEM)
    return pl.pallas_call(
        kernel,
        out_shape=outs,
        in_specs=specs,
        out_specs=[vmem] * len(outs),
        scratch_shapes=scratch,
        compiler_params=pltpu.CompilerParams(vmem_limit_bytes=30 * 2**20),
        cost_estimate=pl.CostEstimate(flops=flops, bytes_accessed=size, transcendentals=0),
    )(*args)


def shape(dims, dtype=F32):
    return jax.ShapeDtypeStruct(dims, dtype)


def kept(dims, dtype=F32):
    return pltpu.VMEM(dims, dtype)


def exchange(blocks, axes=AXES):
    return lax.all_to_all(blocks, axes, 0, 0, tiled=True)


def exchange_rows(rows, axes=AXES):
    return exchange(rows[:, None, :], axes)[:, 0, :]


def shards(spectrum, clip_bounds, kernel_one, gain_one, bias_one, kernel_two, gain_two, bias_two, pooled_grad):
    _, rows, frame_dev = spectrum.shape
    chan = kernel_two.shape[0]
    n_mel, n_tm = lax.axis_size("mel"), lax.axis_size("tm")
    devices = n_mel * n_tm
    half = frame_dev // 2
    wide = frame_dev + RIM
    mels = n_mel * rows

    packed, own = run(
        pack_mel,
        [kept((n_mel, 2 * rows + chan, half), BF16), kept((chan * rows // 2, half), BF16)],
        [
            pltpu.VMEM(spectrum.shape, BF16),
            pltpu.VMEM(pooled_grad.shape, BF16),
            pltpu.SemaphoreType.DMA((2,)),
        ],
        spectrum,
        pooled_grad,
        hbm=2,
    )
    recv_mel = exchange(packed, "mel")
    ext = rows + 6
    span = 6 * 3 * chan
    wf, wb, w1, ws, pairs, singles, k1t, params, masks, edge_masks, twice = run(
        weights,
        [
            kept((4 * chan, span), BF16),
            kept((4 * chan, span), BF16),
            kept((ext * chan, 128), BF16),
            kept((rows * 8, (rows + 2) * chan), BF16),
            kept((chan, 128)),
            kept((chan, 128)),
            kept((16, chan)),
            kept((8, chan)),
            kept((8, wide)),
            kept((n_tm * 8, 128)),
            kept((128, 128)),
        ],
        [
            pltpu.VMEM((9, chan, chan), BF16),
            pltpu.VMEM((3, 3, chan), BF16),
            pltpu.VMEM((4, 1, chan), F32),
            pltpu.SemaphoreType.DMA((6,)),
        ],
        clip_bounds,
        jnp.transpose(kernel_two, (2, 3, 0, 1)).reshape(9, chan, chan),
        jnp.transpose(kernel_one, (1, 2, 0)),
        gain_one[None],
        bias_one[None],
        gain_two[None],
        bias_two[None],
        hbm=6,
    )
    (packed,) = run(
        pack_tm,
        [kept((n_tm, 16, 128), BF16)],
        [pltpu.VMEM((n_tm * 16, 128), F32)],
        recv_mel,
        own,
        masks,
    )
    recv_tm = exchange(packed, "tm")
    pre_two, payload, act, pre_one, slope, x3, stats_one, features = run(
        forward_one,
        [
            kept(((rows + 4) * chan, wide)),
            kept((devices, 128)),
            kept((ext * 3 * chan, wide), BF16),
            kept((ext * chan, wide)),
            kept((ext * chan, wide)),
            kept((128, wide), BF16),
            kept((chan + 16, 128)),
            kept((8, 128)),
        ],
        [pltpu.VMEM((mels + 8, wide), F32)],
        recv_mel,
        recv_tm,
        pairs,
        singles,
        twice,
        w1,
        wf,
        params,
        masks,
        edge_masks,
    )
    recv = exchange_rows(payload)
    (up,) = run(
        expand,
        [kept(((rows // 2 + 2) * chan, wide))],
        [pltpu.VMEM((rows // 2 * chan, 128), F32)],
        recv_mel,
        recv_tm,
        own,
    )
    grad, payload, row_pairs, stats_two = run(
        backward_scaled,
        [
            kept(((rows + 4) * chan, wide)),
            kept((devices, 128)),
            kept((rows // 2 * chan, frame_dev)),
            kept((chan, 128)),
        ],
        [],
        recv,
        pre_two,
        up,
        params,
        masks,
    )
    recv = exchange_rows(payload)
    (pooled,) = run(
        pool,
        [shape((1, chan, rows // 2, half), BF16)],
        [pltpu.VMEM((rows // 2 * chan, 128), F32)],
        row_pairs,
    )
    pieces = 9 * chan * chan // 128
    g3, payload, gain_two_grad, bias_two_grad = run(
        backward_two,
        [kept((ext * 3 * chan, wide), BF16), kept((pieces, 128)), shape((1, chan)), shape((1, chan))],
        [pltpu.VMEM(((rows + 4) * chan, frame_dev), BF16)],
        recv,
        pre_two,
        grad,
        stats_two,
        params,
        masks,
        act,
    )
    share = -(-pieces // devices)
    if share * devices > pieces:
        payload = jnp.pad(payload, ((0, share * devices - pieces), (0, 0)))
    recv = exchange_rows(payload)
    g1, sums = run(
        backward_one,
        [kept(((rows + 4) * chan, wide)), kept((8, 128))],
        [],
        wb,
        g3,
        slope,
        x3,
    )
    (payload,) = run(collect, [kept((devices * 14, 128))], [], recv, sums)
    recv = exchange_rows(payload)
    spec_grad, kernel_one_grad, kernel_two_grad, gain_one_grad, bias_one_grad = run(
        finish,
        [
            shape((1, rows, frame_dev)),
            shape((3, 3, chan)),
            shape((9, chan, chan)),
            shape((1, chan)),
            shape((1, chan)),
        ],
        [
            pltpu.VMEM(((rows + 2) * chan, wide), BF16),
            pltpu.VMEM((rows * 8, wide), F32),
            pltpu.VMEM((3, rows * 8, 128), F32),
        ],
        recv,
        features,
        stats_one,
        k1t,
        g1,
        pre_one,
        ws,
        params,
        masks,
    )
    kernel_two_grad = jnp.transpose(kernel_two_grad.reshape(3, 3, chan, chan), (2, 3, 0, 1))
    return (
        pooled,
        spec_grad,
        jnp.transpose(kernel_one_grad, (2, 0, 1)),
        gain_one_grad[0],
        bias_one_grad[0],
        kernel_two_grad,
        gain_two_grad[0],
        bias_two_grad[0],
    )


def solution(mesh):
    return jax.shard_map(
        shards,
        mesh=mesh,
        in_specs=(
            P(None, "mel", "tm"),
            P(),
            P(),
            P(),
            P(),
            P(),
            P(),
            P(),
            P(None, None, "mel", "tm"),
        ),
        out_specs=(P(None, None, "mel", "tm"), P(None, "mel", "tm"), P(), P(), P(), P(), P(), P()),
        check_vma=False,
    )
```

```python
import functools

import jax
import jax.numpy as jnp
from jax import lax
from jax.experimental import pallas as pl
from jax.experimental.pallas import tpu as pltpu
from jax.sharding import PartitionSpec as P

F32 = jnp.float32
BF16 = jnp.bfloat16
AXES = ("mel", "tm")
EXACT = lax.Precision.HIGHEST
RIM = 128
BAND = 24
MEL_ROWS = 16


def iota(shape, dim):
    return lax.broadcasted_iota(jnp.int32, shape, dim)


def dot(a, b, over=((1,), (0,)), precision=None):
    return lax.dot_general(a, b, (over, ((), ())), precision=precision, preferred_element_type=F32)


def to_column(lanes, count, start=0):
    shape = (count, lanes.shape[1])
    return jnp.sum(jnp.where(iota(shape, 1) == iota(shape, 0) + start, lanes, 0.0), axis=1, keepdims=True)


def to_lanes(column, start=0, width=128):
    shape = (column.shape[0], width)
    return jnp.sum(jnp.where(iota(shape, 1) == iota(shape, 0) + start, column, 0.0), axis=0, keepdims=True)


def frame_masks(bounds, frames):
    last = bounds.shape[1] - 1

    def living(f):
        return (f >= 0) & (f < bounds[0, last])

    def paired(f):
        both = living(f) & living(f + 1)
        for k in range(1, last):
            both = both & (f + 1 != bounds[0, k])
        return both

    return tuple(m.astype(F32) for m in (living(frames), paired(frames - 1), paired(frames)))


def row_valid(row, rows):
    mel = lax.axis_index("mel") * rows + row
    return ((mel >= 0) & (mel < lax.axis_size("mel") * rows)).astype(F32)


def load_all(*pairs, sems):
    copies = [pltpu.make_async_copy(src, dst, sems.at[n]) for n, (src, dst) in enumerate(pairs)]
    for copy in copies:
        copy.start()
    for copy in copies:
        copy.wait()


def pack_mel(spec_hbm, grad_hbm, out, own, spec, grad, sems):
    load_all((spec_hbm, spec), (grad_hbm, grad), sems=sems)
    me = lax.axis_index("mel")
    x = spec[0]
    rows, frame_dev = x.shape
    half = frame_dev // 2
    g = grad[0].astype(F32)
    top = g[:, 0, :]
    bottom = g[:, g.shape[1] - 1, :]
    for j in range(out.shape[0]):
        out[j, 0:rows] = x[:, :half]
        out[j, rows : 2 * rows] = x[:, half:]
        edge = jnp.where(j == me - 1, top, 0.0) + jnp.where(j == me + 1, bottom, 0.0)
        out[j, 2 * rows :] = edge.astype(BF16)
    own[...] = g.reshape(own.shape).astype(BF16)


def weights(bounds, k2_hbm, k1_hbm, gain_one_hbm, bias_one_hbm, gain_two_hbm, bias_two_hbm,
            wf, wb, w1, ws, pairs, singles, k1t, params, masks, edge_masks, twice, k2, k1, vectors, sems):
    load_all(
        (k2_hbm, k2),
        (k1_hbm, k1),
        (gain_one_hbm, vectors.at[0]),
        (bias_one_hbm, vectors.at[1]),
        (gain_two_hbm, vectors.at[2]),
        (bias_two_hbm, vectors.at[3]),
        sems=sems,
    )
    chan = k2.shape[1]
    span = wf.shape[1]
    wide = masks.shape[1]
    frame_dev = wide - RIM
    lane = iota((1, wide), 1)
    frames = lax.axis_index("tm") * frame_dev + jnp.where(lane < frame_dev + RIM // 2, lane, lane - wide)
    last = bounds.shape[1] - 1
    pixels = (bounds[0, last] * (lax.axis_size("mel") * MEL_ROWS)).astype(F32)
    masks[...] = jnp.concatenate(
        list(frame_masks(bounds, frames)) + [jnp.full((1, wide), 1.0) * pixels, jnp.zeros((4, wide), F32)], axis=0
    )
    q = iota(edge_masks.shape, 0)
    lane = iota(edge_masks.shape, 1)
    k = q % 8
    frames = (q // 8) * frame_dev + jnp.where(k < 4, k, k + frame_dev - 8)
    living, behind, ahead = frame_masks(bounds, frames)
    living = jnp.where((k == 0) | (k == 7), living, 0.0)
    edge_masks[...] = jnp.where(lane == 0, living, jnp.where(lane == 1, behind, jnp.where(lane == 2, ahead, 0.0)))
    params[...] = jnp.concatenate(
        [vectors[n] for n in range(4)] + [jnp.zeros((4, chan), F32)], axis=0
    )
    tap = iota((16, 128), 0)
    lane = iota((16, 128), 1)
    i = (tap * 11) >> 5
    ninth = (lane * 57) >> 9
    to_band = (lane == BAND * (tap - 3 * i) + i) & (tap < 9)
    to_left = (ninth == tap) & (tap < 9)
    to_right = (lane - 9 * ninth == tap) & (lane < 81)
    to_single = (lane == 81 + tap) & (tap < 9)
    source = iota((128, 128), 0) - 81
    lane = iota((128, 128), 1)
    ninth = (lane * 57) >> 9
    inside = (source >= 0) & (source < 9) & (lane < 81)
    twice[...] = jnp.where(inside, (source == ninth).astype(F32) + (source == lane - 9 * ninth).astype(F32), 0.0)
    taps = [k2[t].astype(F32) for t in range(9)]
    rest = jnp.zeros((chan, span - 9 * chan), F32)
    forward = jnp.concatenate(taps + [rest], axis=1)
    backward = jnp.concatenate([taps[8 - t].T for t in range(9)] + [rest], axis=1)
    for r in range(wf.shape[0] // chan):
        at = slice(r * chan, (r + 1) * chan)
        wf[at] = (pltpu.roll(forward, 3 * chan * r, 1) if r else forward).astype(BF16)
        wb[at] = (pltpu.roll(backward, 3 * chan * r, 1) if r else backward).astype(BF16)
    full = jnp.concatenate([k1[n].astype(F32) for n in range(3)] + [jnp.zeros((7, chan), F32)], axis=0)
    k1t[...] = full
    k = full.astype(BF16)
    lanes = [dot(k, select.astype(BF16), ((0,), (0,))) for select in (to_band, to_left, to_right, to_single)]
    pairs[...] = lanes[1] * lanes[2]
    singles[...] = lanes[3]
    for m in range(w1.shape[0] // chan):
        w1[m * chan : (m + 1) * chan] = (pltpu.roll(lanes[0], m, 1) if m else lanes[0]).astype(BF16)
    low = [
        jnp.concatenate([full[3 * (2 - a) + 2 - b : 3 * (2 - a) + 3 - b] for a in range(3)], axis=1)
        for b in range(3)
    ]
    base = jnp.concatenate(low + [jnp.zeros((5, 3 * chan), F32)], axis=0)
    base = jnp.concatenate([base, jnp.zeros((8, ws.shape[1] - 3 * chan), F32)], axis=1)
    for m in range(ws.shape[0] // 8):
        ws[8 * m : 8 * m + 8] = (pltpu.roll(base, chan * m, 1) if m else base).astype(BF16)


def feature_rows(shifted, axis_shift, weight, centre):
    z = [None] * 9
    for j in range(3):
        for i in range(3):
            z[3 * i + j] = axis_shift(shifted[j], i) - centre

    def folded(v):
        if v.shape[1] > 128:
            v = v[:, :128] + v[:, 128:]
        return jnp.sum(v, axis=0, keepdims=True)

    rows = [None] * 96
    for s in range(9):
        left = z[s] * weight
        rows[81 + s] = folded(left)
        for t in range(s, 9):
            rows[9 * s + t] = rows[9 * t + s] = folded(left * z[t])
    zero = jnp.zeros((1, 128), F32)
    stack = jnp.concatenate([zero if r is None else r for r in rows], axis=0)
    return to_lanes(jnp.sum(stack, axis=1, keepdims=True))


def pack_tm(recv, own, masks, out, spread):
    count = out.shape[0]
    n_mel = recv.shape[0]
    me_m, me_t = lax.axis_index("mel"), lax.axis_index("tm")
    rows = MEL_ROWS
    half = recv.shape[2]
    frame_dev = 2 * half
    mels = n_mel * rows
    lane = iota((1, frame_dev), 1)
    usable, behind, ahead = (masks[n : n + 1, :frame_dev] for n in range(3))
    x = jnp.concatenate(
        [
            jnp.concatenate([recv[j, 0:rows] for j in range(n_mel)], axis=0),
            jnp.concatenate([recv[j, rows : 2 * rows] for j in range(n_mel)], axis=0),
        ],
        axis=1,
    )
    x = x.astype(F32) * usable
    inner = jnp.where((lane > 0) & (lane < frame_dev - 1), usable, 0.0)
    number = mels * jnp.sum(inner, axis=1, keepdims=True)
    centre = jnp.sum(jnp.sum(x, axis=0, keepdims=True), axis=1, keepdims=True)
    centre = centre / (mels * jnp.maximum(jnp.sum(usable, axis=1, keepdims=True), 1.0))
    centre = lax.reduce_precision(centre, 8, 7)
    row = iota((mels, frame_dev), 0)

    def mel_shift(v, i):
        if i == 1:
            return v
        if i == 0:
            return jnp.where(row == 0, 0.0, pltpu.roll(v, 1, 0))
        return jnp.where(row == mels - 1, 0.0, pltpu.roll(v, mels - 1, 0))

    shifted = [pltpu.roll(x, 1, 1) * behind, x, pltpu.roll(x, frame_dev - 1, 1) * ahead]
    features = feature_rows(shifted, mel_shift, inner, centre)
    lane = iota((1, 128), 1)
    features = jnp.where(lane == 90, centre, jnp.where(lane == 91, number, features))
    high = lax.reduce_precision(features, 8, 7)
    mid = lax.reduce_precision(features - high, 8, 7)
    low = features - high - mid
    pick = iota((8, frame_dev), 0)
    column = jnp.where(pick < 4, pick, frame_dev - 8 + pick)
    edges = dot((iota((8, frame_dev), 1) == column).astype(BF16), x.astype(BF16), ((1,), (1,)))
    edges = jnp.concatenate([edges, jnp.zeros((8, 128 - mels), F32)], axis=1)
    target = iota((count, half), 0)
    at = iota((count, half), 1)
    choose = ((target == me_t - 1) & (at == 0)) | ((target == me_t + 1) & (at == half - 1))
    choose = choose.astype(BF16)
    above = recv[jnp.maximum(me_m - 1, 0), 2 * rows :]
    below = recv[jnp.minimum(me_m + 1, n_mel - 1), 2 * rows :]
    columns = dot(choose, own[...], ((1,), (1,)))
    outer = jnp.concatenate([dot(choose, above, ((1,), (1,))), dot(choose, below, ((1,), (1,)))], axis=1)
    parts = columns.shape[1] // 128
    for q in range(parts):
        spread[pl.ds(8 + q, count, stride=16), :] = columns[:, 128 * q : 128 * (q + 1)]
    spread[pl.ds(8 + parts, count, stride=16), :] = outer
    common = jnp.concatenate([high, mid, low], axis=0)
    for j in range(count):
        tail = jnp.concatenate([spread[16 * j + 8 : 16 * j + 13, :], common], axis=0)
        out[j] = jnp.concatenate([edges, tail], axis=0).astype(BF16)


def expand(recv_mel, recv_tm, own, out, temp):
    me_m, me_t = lax.axis_index("mel"), lax.axis_index("tm")
    n_mel, count = recv_mel.shape[0], recv_tm.shape[0]
    half = own.shape[1]
    rows = MEL_ROWS // 2
    chan = own.shape[0] // rows
    wide = out.shape[1]
    above = recv_mel[jnp.maximum(me_m - 1, 0), 2 * MEL_ROWS :]
    below = recv_mel[jnp.minimum(me_m + 1, n_mel - 1), 2 * MEL_ROWS :]
    every = jnp.concatenate([own[...], above, below], axis=0)
    after = recv_tm[jnp.minimum(me_t + 1, count - 1)].astype(F32)
    before = recv_tm[jnp.maximum(me_t - 1, 0)].astype(F32)
    after = jnp.concatenate([after[8 + q : 9 + q] for q in range(5)], axis=1)
    before = jnp.concatenate([before[8 + q : 9 + q] for q in range(5)], axis=1)
    side = iota((16, after.shape[1]), 0)
    sides = jnp.where(side == 0, after, jnp.where(side == 1, before, 0.0)).astype(BF16)
    lane = iota((half, wide), 1)
    spread = jnp.where((lane >> 1 == iota((half, wide), 0)) & (lane < 2 * half), 0.25, 0.0).astype(BF16)
    lane = iota((16, wide), 1)
    side = iota((16, wide), 0)
    right = (side == 0) & (lane >= 2 * half) & (lane < 2 * half + 2)
    left = (side == 1) & (lane >= wide - 2)
    columns = jnp.where(right | left, 0.25, 0.0).astype(BF16)
    full = dot(every, spread) + dot(sides, columns, ((0,), (0,)))
    for part in range(wide // 128):
        cut = slice(128 * part, 128 * (part + 1))
        temp[...] = full[: chan * rows, cut]
        for r in range(rows):
            out[(r + 1) * chan : (r + 2) * chan, cut] = temp[pl.ds(r, chan, stride=rows), :]
    out[0:chan] = full[chan * rows : chan * (rows + 1)]
    out[(rows + 1) * chan :] = full[chan * (rows + 1) :]


def silu_halves(h):
    t = jnp.tanh(h)
    one = 1.0 + t
    return h * one, one * (1.0 + h * (1.0 - t))


def forward_one(recv_mel, recv_tm, pairs, singles, twice, w1, wf, params, masks, edge_masks,
                pre_two, payload, own_act, x3, stats, features_out, act, pre_one, xs):
    n_mel, count = recv_mel.shape[0], recv_tm.shape[0]
    rows = MEL_ROWS
    mels = n_mel * rows
    half = recv_mel.shape[2]
    frame_dev = 2 * half
    wide = frame_dev + RIM
    chan = params.shape[1]
    me_m, me_t = lax.axis_index("mel"), lax.axis_index("tm")
    usable, behind, ahead = (masks[n : n + 1] for n in range(3))
    total = masks[3:4, 0:1]
    x = jnp.concatenate(
        [
            jnp.concatenate([recv_mel[j, 0:rows] for j in range(n_mel)], axis=0),
            jnp.concatenate([recv_mel[j, rows : 2 * rows] for j in range(n_mel)], axis=0),
        ],
        axis=1,
    ).astype(F32)
    after = recv_tm[jnp.minimum(me_t + 1, count - 1)].astype(F32)[0:8, :mels]
    before = recv_tm[jnp.maximum(me_t - 1, 0)].astype(F32)[0:8, :mels]
    after = jnp.where(me_t + 1 < count, after, 0.0)
    before = jnp.where(me_t > 0, before, 0.0)
    sides = jnp.concatenate([after[0:4], before[4:8], jnp.zeros((8, mels), F32)], axis=0).astype(BF16)
    side = iota((16, RIM), 0)
    place = iota((16, RIM), 1) == jnp.where(side < 4, side, jnp.where(side < 8, side + RIM - 8, -1))
    x = jnp.concatenate([x, dot(sides, place.astype(BF16), ((0,), (0,)))], axis=1) * usable
    xs[0:8] = jnp.zeros((8, wide), F32)
    xs[mels : mels + 8] = jnp.zeros((8, wide), F32)
    xs[4 : mels + 4] = x
    near = xs[pl.ds(pl.multiple_of(me_m * rows, 8), BAND), :]
    x3[...] = jnp.concatenate(
        [
            pltpu.roll(near, 1, 1) * behind,
            near,
            pltpu.roll(near, wide - 1, 1) * ahead,
            jnp.broadcast_to(usable, (BAND, wide)),
            jnp.zeros((128 - 4 * BAND, wide), F32),
        ],
        axis=0,
    ).astype(BF16)
    pre_one[...] = dot(w1[...], x3[...])
    parts = [recv_tm[d].astype(F32)[8:16] for d in range(count)]
    parts = [p[5:6] + p[6:7] + p[7:8] for p in parts]
    centres = [p[:, 90:91] for p in parts]
    numbers = [p[:, 91:92] for p in parts]
    weight = functools.reduce(jnp.add, numbers)
    centre = functools.reduce(jnp.add, [c * n for c, n in zip(centres, numbers)]) / jnp.maximum(weight, 1.0)
    lane = iota((1, 128), 1)
    features = jnp.zeros((1, 128), F32)
    moved = jnp.zeros((1, 128), F32)
    for part, c, n in zip(parts, centres, numbers):
        delta = c - centre
        moved = moved + delta * part
        features = features + part + delta * n * jnp.where(lane < 81, delta, 1.0)
    moved = dot(jnp.broadcast_to(moved, (8, 128)), twice[...], precision=EXACT)[0:1]
    features = features + moved
    edge = recv_tm[:, 0:8, :].astype(F32).reshape(count * 8, 128)
    q_usable, q_behind, q_ahead = (edge_masks[:, n : n + 1] for n in range(3))
    lane = iota((count * 8, 128), 1)

    def lane_shift(v, i):
        if i == 1:
            return v
        if i == 0:
            return jnp.where(lane < mels, pltpu.roll(v, 1, 1), 0.0)
        return pltpu.roll(v, 127, 1)

    shifted = [
        pltpu.roll(edge, 1, 0) * q_behind,
        edge,
        pltpu.roll(edge, count * 8 - 1, 0) * q_ahead,
    ]
    features = features + feature_rows(shifted, lane_shift, jnp.where(lane < mels, q_usable, 0.0), centre)
    features = jnp.where(iota((1, 128), 1) < 90, features, 0.0)
    features_out[...] = jnp.concatenate(
        [features, jnp.broadcast_to(centre, (1, 128)), jnp.zeros((6, 128), F32)], axis=0
    )
    near_mean = jnp.sum(singles[...] * features, axis=1, keepdims=True) / total
    square = jnp.sum(pairs[...] * features, axis=1, keepdims=True) / total
    inv = lax.rsqrt(square - near_mean * near_mean + 1e-05)
    mean = near_mean + centre * jnp.sum(singles[...], axis=1, keepdims=True)
    lane = iota((chan, 128), 1)
    stats[0:chan] = jnp.where(lane == 0, mean, jnp.where(lane == 1, inv, 0.0))
    stats[chan : chan + 8] = jnp.broadcast_to(to_lanes(near_mean), (8, 128))
    stats[chan + 8 : chan + 16] = jnp.broadcast_to(to_lanes(inv), (8, 128))
    scale = 0.5 * to_column(params[0:1], chan) * inv
    shift = 0.5 * to_column(params[1:2], chan) - mean * scale
    stats[chan + 16 :] = jnp.where(lane == 0, scale, jnp.where(lane == 1, shift, 0.0))
    scale = jnp.broadcast_to(scale, (chan, wide))
    shift = jnp.broadcast_to(shift, (chan, wide))
    ext = w1.shape[0] // chan

    def row_step(r, carry):
        at = pl.ds(pl.multiple_of(r * chan, chan), chan)
        value, _ = silu_halves(pre_one[at, :] * scale + shift)
        value = value * (usable * row_valid(r - 3, rows))
        base = pl.multiple_of(r * 3 * chan, chan)
        act[pl.ds(base, chan), :] = (pltpu.roll(value, 1, 1) * behind).astype(BF16)
        act[pl.ds(base + chan, chan), :] = value.astype(BF16)
        act[pl.ds(base + 2 * chan, chan), :] = (pltpu.roll(value, wide - 1, 1) * ahead).astype(BF16)
        return carry

    lax.fori_loop(0, ext, row_step, 0)
    for m in range(rows + 2):
        own_act[m * chan : (m + 1) * chan] = act[(3 * m + 7) * chan : (3 * m + 8) * chan, :frame_dev]
    first = jnp.zeros((chan, frame_dev), F32)
    second = jnp.zeros((chan, frame_dev), F32)
    taps = wf.shape[1]
    for g in range(pre_two.shape[0] // wf.shape[0]):
        at = slice(g * wf.shape[0], (g + 1) * wf.shape[0])
        start = g * 3 * wf.shape[0]
        pre_two[at] = dot(wf[...], act[start : start + taps, :])

    def sum_step(q, carry):
        one, two = carry
        p = pre_two[pl.ds(pl.multiple_of(q * chan, chan), chan), :frame_dev]
        masked = p * usable[:, :frame_dev]
        return one + masked, two + masked * p

    first, second = lax.fori_loop(2, 2 + rows, sum_step, (first, second))
    first = jnp.sum(first, axis=1, keepdims=True)
    second = jnp.sum(second, axis=1, keepdims=True)
    payload[...] = jnp.broadcast_to(to_lanes(first) + to_lanes(second, chan), payload.shape)


def backward_scaled(recv, pre_two, recv_mel, recv_tm, pooled_own, params, masks, grad, payload, pairs, stats, up, temp):
    expand(recv_mel, recv_tm, pooled_own, up, temp)
    chan = params.shape[1]
    rows = MEL_ROWS
    wide = pre_two.shape[1]
    frame_dev = wide - RIM
    usable = masks[0:1]
    total = masks[3:4, 0:1]
    sums = jnp.sum(recv[...], axis=0, keepdims=True)
    mean = to_column(sums, chan) / total
    inv = lax.rsqrt(to_column(sums, chan, chan) / total - mean * mean + 1e-05)
    lane = iota((chan, 128), 1)
    stats[...] = jnp.where(lane == 0, mean, jnp.where(lane == 1, inv, 0.0))
    mean = jnp.broadcast_to(mean, (chan, wide))
    inv = jnp.broadcast_to(inv, (chan, wide))
    scale = 0.5 * to_column(params[2:3], chan)
    shift = jnp.broadcast_to(0.5 * to_column(params[3:4], chan), (chan, wide))
    scale = jnp.broadcast_to(scale, (chan, wide))

    def pair(r, carry, own):
        upstream = up[pl.ds(pl.multiple_of(r * chan, chan), chan), :]
        both = None
        for h in range(2):
            q = 2 * r + h
            at = pl.ds(pl.multiple_of(q * chan, chan), chan)
            mask = usable * row_valid(q - 2, rows)
            normed = (pre_two[at, :] - mean) * inv
            value, slope = silu_halves(normed * scale + shift)
            g = upstream * slope * (0.5 * mask)
            grad[at, :] = g
            if own:
                g = g[:, :frame_dev]
                carry = (carry[0] + g * normed[:, :frame_dev], carry[1] + g)
                value = value[:, :frame_dev] * usable[:, :frame_dev]
                both = value if h == 0 else both + value
        if own:
            pairs[pl.ds(pl.multiple_of((r - 1) * chan, chan), chan), :] = both
        return carry

    zero = jnp.zeros((chan, frame_dev), F32)
    pair(0, None, False)
    last = up.shape[0] // chan - 1
    pair(last, None, False)
    first, second = lax.fori_loop(1, last, lambda r, c: pair(r, c, True), (zero, zero))
    first = jnp.sum(first, axis=1, keepdims=True)
    second = jnp.sum(second, axis=1, keepdims=True)
    payload[...] = jnp.broadcast_to(to_lanes(first) + to_lanes(second, chan), payload.shape)


def pool(pairs, after, out, temp):
    del after
    chan, rows, half = out.shape[1:]
    to_mean = jnp.where(iota((2 * half, half), 0) >> 1 == iota((2 * half, half), 1), 0.25, 0.0)
    pooled = dot(pairs[...], to_mean, precision=EXACT)
    for r in range(rows):
        temp[pl.ds(r, chan, stride=rows), :] = pooled[r * chan : (r + 1) * chan]
    out[0] = temp[...].reshape(chan, rows, half).astype(BF16)


def backward_two(recv, pre_two, grad, stats, params, masks, act, out, payload, gain_out, bias_out, shifted):
    chan = params.shape[1]
    rows = MEL_ROWS
    wide = pre_two.shape[1]
    frame_dev = wide - RIM
    usable, behind, ahead = (masks[n : n + 1] for n in range(3))
    behind, ahead = behind[:, :frame_dev], ahead[:, :frame_dev]
    total = masks[3:4, 0:1]
    sums = jnp.sum(recv[...], axis=0, keepdims=True)
    gain_out[...] = sums[:, :chan]
    bias_out[...] = sums[:, chan:]
    mean, inv = stats[:, 0:1], stats[:, 1:2]
    factor = to_column(params[2:3], chan) * inv
    gain_part = jnp.broadcast_to(to_column(sums, chan) / total * inv, (chan, wide))
    bias_part = jnp.broadcast_to(to_column(sums, chan, chan) / total, (chan, wide))
    mean = jnp.broadcast_to(mean, (chan, wide))
    factor = jnp.broadcast_to(factor, (chan, wide))
    count = pre_two.shape[0] // chan

    def row(q, own):
        at = pl.ds(pl.multiple_of(q * chan, chan), chan)
        mask = usable * row_valid(q - 2, rows)
        centred = grad[at, :] - (bias_part + (pre_two[at, :] - mean) * gain_part) * mask
        value = factor * centred
        low = value.astype(BF16)
        out[at, :] = low
        if own:
            base = pl.multiple_of((q - 2) * 3 * chan, chan)
            shifted[pl.ds(base, chan), :] = (pltpu.roll(value, 1, 1)[:, :frame_dev] * behind).astype(BF16)
            shifted[pl.ds(base + chan, chan), :] = low[:, :frame_dev]
            shifted[pl.ds(base + 2 * chan, chan), :] = (
                pltpu.roll(value, wide - 1, 1)[:, :frame_dev] * ahead
            ).astype(BF16)
        return 0

    for q in (0, 1, count - 2, count - 1):
        row(q, False)
    lax.fori_loop(2, count - 2, lambda q, c: row(q, True), 0)
    table = jnp.zeros((3 * chan, 3 * chan), F32)
    for m in range(rows):
        left = shifted[m * 3 * chan : (m + 1) * 3 * chan, :]
        table = table + dot(left, act[m * chan : (m + 3) * chan, :], ((1,), (1,)))
    payload[0 : 3 * chan] = table[:, :128]
    upper = 3 * chan // 2
    payload[3 * chan :] = jnp.concatenate([table[:upper, 128:], table[upper:, 128:]], axis=1)


def backward_one(wb, grad, w1, x3, stats, masks, g1, sums, g3, pre_one):
    chan = wb.shape[0] // 4
    rows = MEL_ROWS
    wide = x3.shape[1]
    frame_dev = wide - RIM
    usable, behind, ahead = (masks[n : n + 1] for n in range(3))
    block = wb.shape[0]
    count = grad.shape[0] // chan
    pre_one[...] = dot(w1[2 * chan : (rows + 4) * chan], x3[...])

    def shift_step(q, carry):
        at = pl.ds(pl.multiple_of(q * chan, chan), chan)
        low = grad[at, :]
        value = low.astype(F32)
        base = pl.multiple_of(q * 3 * chan, chan)
        g3[pl.ds(base, chan), :] = (pltpu.roll(value, 1, 1) * behind).astype(BF16)
        g3[pl.ds(base + chan, chan), :] = low
        g3[pl.ds(base + 2 * chan, chan), :] = (pltpu.roll(value, wide - 1, 1) * ahead).astype(BF16)
        return carry

    lax.fori_loop(0, count, shift_step, 0)
    for start in range(0, rows + 2, 4):
        step = min(4, rows + 2 - start)
        g1[start * chan : (start + step) * chan] = dot(
            wb[: step * chan, : (step + 2) * 3 * chan], g3[start * 3 * chan : (start + step + 2) * 3 * chan, :]
        )
    scale = jnp.broadcast_to(stats[chan + 16 :, 0:1], (chan, wide))
    shift = jnp.broadcast_to(stats[chan + 16 :, 1:2], (chan, wide))

    def slope_step(q, carry):
        at = pl.ds(pl.multiple_of(q * chan, chan), chan)
        _, slope = silu_halves(pre_one[at, :] * scale + shift)
        g1[at, :] = g1[at, :] * slope * (0.5 * usable * row_valid(q - 1, rows))
        return carry

    lax.fori_loop(0, rows + 2, slope_step, 0)
    table = jnp.zeros((chan, 128), F32)
    for g in range(rows // 4):
        part = g1[chan + g * block : chan + (g + 1) * block, :frame_dev]
        high = lax.reduce_precision(part, 8, 7)
        low = (part - high).astype(BF16)
        taps_in = x3[:, :frame_dev]
        products = dot(high.astype(BF16), taps_in, ((1,), (1,))) + dot(low, taps_in, ((1,), (1,)))
        for m in range(4):
            table = table + pltpu.roll(products[m * chan : (m + 1) * chan], 128 - (4 * g + m + 3), 1)
    tap = iota((16, 128), 0)
    lane = iota((16, 128), 1)
    i = (tap * 11) >> 5
    select = ((lane == BAND * (tap - 3 * i) + i) & (tap < 9)) | ((lane == 3 * BAND) & (tap == 9))
    rows10 = dot(select.astype(F32), table, ((1,), (1,)), EXACT)
    sums[...] = jnp.concatenate(
        [jnp.concatenate([rows10[0:5], rows10[5:10]], axis=1), jnp.zeros((3, 128), F32)], axis=0
    )


def collect(recv, sums, out):
    count = out.shape[0] // 14
    share = recv.shape[0] // count
    mine = recv[0:share, :]
    for d in range(1, count):
        mine = mine + recv[share * d : share * (d + 1), :]
    block = jnp.concatenate([sums[0:5], mine] + [jnp.zeros((9 - share, 128), F32)] * (share < 9), axis=0)
    for d in range(count):
        out[14 * d : 14 * (d + 1), :] = block


def finish(recv, features, stats, k1t, g1, w1, x3, ws, params, masks,
           spec_grad, kernel_one, kernel_two, gain_out, bias_out, low, taps_out, table, pre_one):
    chan = params.shape[1]
    rows = MEL_ROWS
    wide = g1.shape[1]
    frame_dev = wide - RIM
    usable, behind, ahead = (masks[n : n + 1] for n in range(3))
    total = masks[3:4, 0:1]
    gain = params[0:1]
    count = recv.shape[0] // 14
    share = -(-9 * chan * chan // 128 // count)
    sums = recv[0:5, :]
    for d in range(1, count):
        sums = sums + recv[14 * d : 14 * d + 5, :]
    ten = jnp.concatenate([sums[:, :chan], sums[:, chan:]], axis=0)
    bias_sum = ten[9:10]
    mean_l, inv_l = stats[chan : chan + 1, :chan], stats[chan + 8 : chan + 9, :chan]
    pre_one[...] = dot(w1[2 * chan : (rows + 4) * chan], x3[...])
    ten = ten - features[1:2, 0:1] * bias_sum
    k = k1t[0:9]
    gain_sum = inv_l * (jnp.sum(k * ten[0:9], axis=0, keepdims=True) - mean_l * bias_sum)
    gain_out[...] = gain_sum
    bias_out[...] = bias_sum
    row = features[0:1, :]
    lane = iota((1, 128), 1)
    gram = jnp.concatenate(
        [jnp.where(lane < 9, pltpu.roll(row, 128 - 9 * t, 1) if t else row, 0.0) for t in range(9)]
        + [jnp.zeros((7, 128), F32)],
        axis=0,
    )
    single = to_column(row, 16, 81)[0:9]
    k_rows = jnp.concatenate([k1t[...], jnp.zeros((112, chan), F32)], axis=0)
    normed_taps = inv_l * (dot(gram, k_rows, precision=EXACT)[0:9] - single * mean_l)
    factor_l = gain * inv_l
    grad_taps = factor_l * (ten[0:9] - (bias_sum * single + gain_sum * normed_taps) / total)
    for i in range(3):
        kernel_one[i] = grad_taps[3 * i : 3 * i + 3]
    mean, inv = stats[0:chan, 0:1], stats[0:chan, 1:2]
    factor = jnp.broadcast_to(to_column(gain, chan) * inv, (chan, wide))
    gain_part = jnp.broadcast_to(to_column(gain_sum, chan) / total * inv, (chan, wide))
    bias_part = jnp.broadcast_to(to_column(bias_sum, chan) / total, (chan, wide))
    mean = jnp.broadcast_to(mean, (chan, wide))

    def row_step(q, carry):
        at = pl.ds(pl.multiple_of(q * chan, chan), chan)
        mask = usable * row_valid(q - 1, rows)
        centred = g1[at, :] - (bias_part + (pre_one[at, :] - mean) * gain_part) * mask
        low[at, :] = (factor * centred).astype(BF16)
        return carry

    lax.fori_loop(0, rows + 2, row_step, 0)
    taps_out[...] = dot(ws[...], low[...])
    for part in range(3):
        cut = slice(128 * part, 128 * (part + 1))
        table[part] = taps_out[:, cut]
    moved = [
        jnp.concatenate([table[part, pl.ds(b, rows, stride=8), :] for part in range(3)], axis=1) for b in range(3)
    ]
    result = pltpu.roll(moved[0], 1, 1) * behind + moved[1] + pltpu.roll(moved[2], wide - 1, 1) * ahead
    spec_grad[0] = (result * usable)[:, :frame_dev]
    whole = jnp.concatenate([recv[14 * d + 5 : 14 * d + 5 + share, :] for d in range(count)], axis=0)
    upper = 3 * chan // 2
    main = whole[: 3 * chan]
    rest = whole[3 * chan : 3 * chan + upper]
    last = jnp.concatenate([rest[:, :chan], rest[:, chan:]], axis=0)
    for j in range(3):
        at = slice((2 - j) * chan, (3 - j) * chan)
        kernel_two[j] = main[at, :chan]
        kernel_two[3 + j] = main[at, chan:]
        kernel_two[6 + j] = last[at]


def run(kernel, outs, scratch, *args, hbm=0, flops=10**8, size=4 * 10**6):
    vmem = pl.BlockSpec(memory_space=pltpu.VMEM)
    specs = []
    args = list(args)
    for n, a in enumerate(args):
        if a.dtype == jnp.int32:
            specs.append(pl.BlockSpec(memory_space=pltpu.SMEM))
        elif hbm and n >= len(args) - hbm:
            specs.append(pl.BlockSpec(memory_space=pltpu.HBM))
            args[n] = pltpu.with_memory_space_constraint(a, pltpu.HBM)
        else:
            specs.append(vmem)
            args[n] = pltpu.with_memory_space_constraint(a, pltpu.VMEM)
    return pl.pallas_call(
        kernel,
        out_shape=outs,
        in_specs=specs,
        out_specs=[vmem] * len(outs),
        scratch_shapes=scratch,
        compiler_params=pltpu.CompilerParams(vmem_limit_bytes=30 * 2**20),
        cost_estimate=pl.CostEstimate(flops=flops, bytes_accessed=size, transcendentals=0),
    )(*args)


def shape(dims, dtype=F32):
    return jax.ShapeDtypeStruct(dims, dtype)


def kept(dims, dtype=F32):
    return pltpu.VMEM(dims, dtype)


def exchange(blocks, axes=AXES):
    return lax.all_to_all(blocks, axes, 0, 0, tiled=True)


def exchange_rows(rows, axes=AXES):
    return exchange(rows[:, None, :], axes)[:, 0, :]


def shards(spectrum, clip_bounds, kernel_one, gain_one, bias_one, kernel_two, gain_two, bias_two, pooled_grad):
    _, rows, frame_dev = spectrum.shape
    chan = kernel_two.shape[0]
    n_mel, n_tm = lax.axis_size("mel"), lax.axis_size("tm")
    devices = n_mel * n_tm
    half = frame_dev // 2
    wide = frame_dev + RIM
    mels = n_mel * rows

    packed, own = run(
        pack_mel,
        [kept((n_mel, 2 * rows + chan, half), BF16), kept((chan * rows // 2, half), BF16)],
        [
            pltpu.VMEM(spectrum.shape, BF16),
            pltpu.VMEM(pooled_grad.shape, BF16),
            pltpu.SemaphoreType.DMA((2,)),
        ],
        spectrum,
        pooled_grad,
        hbm=2,
    )
    recv_mel = exchange(packed, "mel")
    ext = rows + 6
    span = 6 * 3 * chan
    wf, wb, w1, ws, pairs, singles, k1t, params, masks, edge_masks, twice = run(
        weights,
        [
            kept((4 * chan, span), BF16),
            kept((4 * chan, span), BF16),
            kept((ext * chan, 128), BF16),
            kept((rows * 8, (rows + 2) * chan), BF16),
            kept((chan, 128)),
            kept((chan, 128)),
            kept((16, chan)),
            kept((8, chan)),
            kept((8, wide)),
            kept((n_tm * 8, 128)),
            kept((128, 128)),
        ],
        [
            pltpu.VMEM((9, chan, chan), BF16),
            pltpu.VMEM((3, 3, chan), BF16),
            pltpu.VMEM((4, 1, chan), F32),
            pltpu.SemaphoreType.DMA((6,)),
        ],
        clip_bounds,
        jnp.transpose(kernel_two, (2, 3, 0, 1)).reshape(9, chan, chan),
        jnp.transpose(kernel_one, (1, 2, 0)),
        gain_one[None],
        bias_one[None],
        gain_two[None],
        bias_two[None],
        hbm=6,
    )
    (packed,) = run(
        pack_tm,
        [kept((n_tm, 16, 128), BF16)],
        [pltpu.VMEM((n_tm * 16, 128), F32)],
        recv_mel,
        own,
        masks,
    )
    recv_tm = exchange(packed, "tm")
    pre_two, payload, act, x3, stats_one, features = run(
        forward_one,
        [
            kept(((rows + 4) * chan, wide)),
            kept((devices, 128)),
            kept(((rows + 2) * chan, frame_dev), BF16),
            kept((128, wide), BF16),
            kept((2 * chan + 16, 128)),
            kept((8, 128)),
        ],
        [
            pltpu.VMEM((ext * 3 * chan, wide), BF16),
            pltpu.VMEM((ext * chan, wide), F32),
            pltpu.VMEM((mels + 8, wide), F32),
        ],
        recv_mel,
        recv_tm,
        pairs,
        singles,
        twice,
        w1,
        wf,
        params,
        masks,
        edge_masks,
    )
    recv = exchange_rows(payload)
    grad, payload, row_pairs, stats_two = run(
        backward_scaled,
        [
            kept(((rows + 4) * chan, wide)),
            kept((devices, 128)),
            kept((rows // 2 * chan, frame_dev)),
            kept((chan, 128)),
        ],
        [pltpu.VMEM(((rows // 2 + 2) * chan, wide), F32), pltpu.VMEM((rows // 2 * chan, 128), F32)],
        recv,
        pre_two,
        recv_mel,
        recv_tm,
        own,
        params,
        masks,
    )
    recv = exchange_rows(payload)
    pieces = 9 * chan * chan // 128
    grad, payload, gain_two_grad, bias_two_grad = run(
        backward_two,
        [kept(((rows + 4) * chan, wide), BF16), kept((pieces, 128)), shape((1, chan)), shape((1, chan))],
        [pltpu.VMEM((rows * 3 * chan, frame_dev), BF16)],
        recv,
        pre_two,
        grad,
        stats_two,
        params,
        masks,
        act,
    )
    share = -(-pieces // devices)
    if share * devices > pieces:
        payload = jnp.pad(payload, ((0, share * devices - pieces), (0, 0)))
    recv = exchange_rows(payload)
    g1, sums = run(
        backward_one,
        [kept(((rows + 2) * chan, wide)), kept((8, 128))],
        [pltpu.VMEM(((rows + 4) * 3 * chan, wide), BF16), pltpu.VMEM(((rows + 2) * chan, wide), F32)],
        wb,
        grad,
        w1,
        x3,
        stats_one,
        masks,
    )
    (payload,) = run(collect, [kept((devices * 14, 128))], [], recv, sums)
    recv = exchange_rows(payload)
    (pooled,) = run(
        pool,
        [shape((1, chan, rows // 2, half), BF16)],
        [pltpu.VMEM((rows // 2 * chan, 128), F32)],
        row_pairs,
        sums,
    )
    spec_grad, kernel_one_grad, kernel_two_grad, gain_one_grad, bias_one_grad = run(
        finish,
        [
            shape((1, rows, frame_dev)),
            shape((3, 3, chan)),
            shape((9, chan, chan)),
            shape((1, chan)),
            shape((1, chan)),
        ],
        [
            pltpu.VMEM(((rows + 2) * chan, wide), BF16),
            pltpu.VMEM((rows * 8, wide), F32),
            pltpu.VMEM((3, rows * 8, 128), F32),
            pltpu.VMEM(((rows + 2) * chan, wide), F32),
        ],
        recv,
        features,
        stats_one,
        k1t,
        g1,
        w1,
        x3,
        ws,
        params,
        masks,
    )
    kernel_two_grad = jnp.transpose(kernel_two_grad.reshape(3, 3, chan, chan), (2, 3, 0, 1))
    return (
        pooled,
        spec_grad,
        jnp.transpose(kernel_one_grad, (2, 0, 1)),
        gain_one_grad[0],
        bias_one_grad[0],
        kernel_two_grad,
        gain_two_grad[0],
        bias_two_grad[0],
    )


def solution(mesh):
    return jax.shard_map(
        shards,
        mesh=mesh,
        in_specs=(
            P(None, "mel", "tm"),
            P(),
            P(),
            P(),
            P(),
            P(),
            P(),
            P(),
            P(None, None, "mel", "tm"),
        ),
        out_specs=(P(None, None, "mel", "tm"), P(None, "mel", "tm"), P(), P(), P(), P(), P(), P()),
        check_vma=False,
    )
```

```python
import functools

import jax
import jax.numpy as jnp
from jax import lax
from jax.experimental import pallas as pl
from jax.experimental.pallas import tpu as pltpu
from jax.sharding import PartitionSpec as P

F32 = jnp.float32
BF16 = jnp.bfloat16
AXES = ("mel", "tm")
EXACT = lax.Precision.HIGHEST
RIM = 128
BAND = 24
MEL_ROWS = 16


def iota(shape, dim):
    return lax.broadcasted_iota(jnp.int32, shape, dim)


def dot(a, b, over=((1,), (0,)), precision=None):
    return lax.dot_general(a, b, (over, ((), ())), precision=precision, preferred_element_type=F32)


def to_column(lanes, count, start=0):
    shape = (count, lanes.shape[1])
    return jnp.sum(jnp.where(iota(shape, 1) == iota(shape, 0) + start, lanes, 0.0), axis=1, keepdims=True)


def to_lanes(column, start=0, width=128):
    shape = (column.shape[0], width)
    return jnp.sum(jnp.where(iota(shape, 1) == iota(shape, 0) + start, column, 0.0), axis=0, keepdims=True)


def halves(v):
    return sum(v[:, n : n + 128] for n in range(128, v.shape[1], 128)) + v[:, :128]


def frame_masks(bounds, frames):
    last = bounds.shape[1] - 1

    def living(f):
        return (f >= 0) & (f < bounds[0, last])

    def paired(f):
        both = living(f) & living(f + 1)
        for k in range(1, last):
            both = both & (f + 1 != bounds[0, k])
        return both

    return tuple(m.astype(F32) for m in (living(frames), paired(frames - 1), paired(frames)))


def row_valid(row, rows):
    mel = lax.axis_index("mel") * rows + row
    return ((mel >= 0) & (mel < lax.axis_size("mel") * rows)).astype(F32)


def load_all(*pairs, sems):
    copies = [pltpu.make_async_copy(src, dst, sems.at[n]) for n, (src, dst) in enumerate(pairs)]
    for copy in copies:
        copy.start()
    for copy in copies:
        copy.wait()


def pack_mel(spec_hbm, grad_hbm, out, own, spec, grad, sems):
    load_all((spec_hbm, spec), (grad_hbm, grad), sems=sems)
    me = lax.axis_index("mel")
    x = spec[0]
    rows, frame_dev = x.shape
    half = frame_dev // 2
    g = grad[0].astype(F32)
    top = g[:, 0, :]
    bottom = g[:, g.shape[1] - 1, :]
    for j in range(out.shape[0]):
        out[j, 0:rows] = x[:, :half]
        out[j, rows : 2 * rows] = x[:, half:]
        edge = jnp.where(j == me - 1, top, 0.0) + jnp.where(j == me + 1, bottom, 0.0)
        out[j, 2 * rows :] = edge.astype(BF16)
    own[...] = g.reshape(own.shape).astype(BF16)


def weights(bounds_hbm, k2_hbm, k1_hbm, gain_one_hbm, bias_one_hbm, gain_two_hbm, bias_two_hbm,
            wf, wb_hbm, w1, ws_hbm, pairs, singles, k1t, params, masks, edge_masks, twice,
            k2, k1, vectors, bounds, wb, ws, sems):
    load_all(
        (bounds_hbm, bounds),
        (k2_hbm, k2),
        (k1_hbm, k1),
        (gain_one_hbm, vectors.at[0]),
        (bias_one_hbm, vectors.at[1]),
        (gain_two_hbm, vectors.at[2]),
        (bias_two_hbm, vectors.at[3]),
        sems=sems,
    )
    chan = k2.shape[1]
    span = wf.shape[1]
    wide = masks.shape[1]
    frame_dev = wide - RIM
    lane = iota((1, wide), 1)
    frames = lax.axis_index("tm") * frame_dev + jnp.where(lane < frame_dev + RIM // 2, lane, lane - wide)
    last = bounds.shape[1] - 1
    pixels = (bounds[0, last] * (lax.axis_size("mel") * MEL_ROWS)).astype(F32)
    masks[...] = jnp.concatenate(
        list(frame_masks(bounds, frames)) + [jnp.full((1, wide), 1.0) * pixels, jnp.zeros((4, wide), F32)], axis=0
    )
    q = iota(edge_masks.shape, 0)
    lane = iota(edge_masks.shape, 1)
    k = q % 8
    frames = (q // 8) * frame_dev + jnp.where(k < 4, k, k + frame_dev - 8)
    living, behind, ahead = frame_masks(bounds, frames)
    living = jnp.where((k == 0) | (k == 7), living, 0.0)
    edge_masks[...] = jnp.where(lane == 0, living, jnp.where(lane == 1, behind, jnp.where(lane == 2, ahead, 0.0)))
    params[...] = jnp.concatenate(
        [vectors[n] for n in range(4)] + [jnp.zeros((4, chan), F32)], axis=0
    )
    tap = iota((16, 128), 0)
    lane = iota((16, 128), 1)
    i = (tap * 11) >> 5
    ninth = (lane * 57) >> 9
    to_band = (lane == BAND * (tap - 3 * i) + i) & (tap < 9)
    to_left = (ninth == tap) & (tap < 9)
    to_right = (lane - 9 * ninth == tap) & (lane < 81)
    to_single = (lane == 81 + tap) & (tap < 9)
    source = iota((128, 128), 0) - 81
    lane = iota((128, 128), 1)
    ninth = (lane * 57) >> 9
    inside = (source >= 0) & (source < 9) & (lane < 81)
    twice[...] = jnp.where(inside, (source == ninth).astype(F32) + (source == lane - 9 * ninth).astype(F32), 0.0)
    taps = [k2[t].astype(F32) for t in range(9)]
    rest = jnp.zeros((chan, span - 9 * chan), F32)
    forward = jnp.concatenate(taps + [rest], axis=1)
    backward = jnp.concatenate([taps[8 - t].T for t in range(9)] + [rest], axis=1)
    for r in range(wb.shape[0] // chan):
        at = slice(r * chan, (r + 1) * chan)
        wb[at] = (pltpu.roll(backward, 3 * chan * r, 1) if r else backward).astype(BF16)
    store_wb = pltpu.make_async_copy(wb, wb_hbm, sems.at[7])
    store_wb.start()
    for r in range(wf.shape[0] // chan):
        at = slice(r * chan, (r + 1) * chan)
        wf[at] = (pltpu.roll(forward, 3 * chan * r, 1) if r else forward).astype(BF16)
    full = jnp.concatenate([k1[n].astype(F32) for n in range(3)] + [jnp.zeros((7, chan), F32)], axis=0)
    k1t[...] = full
    k = full.astype(BF16)
    lanes = [dot(k, select.astype(BF16), ((0,), (0,))) for select in (to_band, to_left, to_right, to_single)]
    pairs[...] = lanes[1] * lanes[2]
    singles[...] = lanes[3]
    for m in range(w1.shape[0] // chan):
        w1[m * chan : (m + 1) * chan] = (pltpu.roll(lanes[0], m, 1) if m else lanes[0]).astype(BF16)
    low = [
        jnp.concatenate([full[3 * (2 - a) + 2 - b : 3 * (2 - a) + 3 - b] for a in range(3)], axis=1)
        for b in range(3)
    ]
    base = jnp.concatenate(low + [jnp.zeros((5, 3 * chan), F32)], axis=0)
    base = jnp.concatenate([base, jnp.zeros((8, ws.shape[1] - 3 * chan), F32)], axis=1)
    for m in range(ws.shape[0] // 8):
        ws[8 * m : 8 * m + 8] = (pltpu.roll(base, chan * m, 1) if m else base).astype(BF16)
    store_ws = pltpu.make_async_copy(ws, ws_hbm, sems.at[8])
    store_ws.start()
    store_wb.wait()
    store_ws.wait()


def feature_rows(shifted, axis_shift, weight, centre):
    z = [None] * 9
    for j in range(3):
        for i in range(3):
            z[3 * i + j] = axis_shift(shifted[j], i) - centre

    def folded(v):
        if v.shape[1] > 128:
            v = v[:, :128] + v[:, 128:]
        return jnp.sum(v, axis=0, keepdims=True)

    rows = [None] * 96
    for s in range(9):
        left = z[s] * weight
        rows[81 + s] = folded(left)
        for t in range(s, 9):
            rows[9 * s + t] = rows[9 * t + s] = folded(left * z[t])
    zero = jnp.zeros((1, 128), F32)
    stack = jnp.concatenate([zero if r is None else r for r in rows], axis=0)
    return to_lanes(jnp.sum(stack, axis=1, keepdims=True))


def pack_tm(recv, own, masks, out, spread):
    count = out.shape[0]
    n_mel = recv.shape[0]
    me_m, me_t = lax.axis_index("mel"), lax.axis_index("tm")
    rows = MEL_ROWS
    half = recv.shape[2]
    frame_dev = 2 * half
    mels = n_mel * rows
    lane = iota((1, frame_dev), 1)
    usable, behind, ahead = (masks[n : n + 1, :frame_dev] for n in range(3))
    x = jnp.concatenate(
        [
            jnp.concatenate([recv[j, 0:rows] for j in range(n_mel)], axis=0),
            jnp.concatenate([recv[j, rows : 2 * rows] for j in range(n_mel)], axis=0),
        ],
        axis=1,
    )
    x = x.astype(F32) * usable
    inner = jnp.where((lane > 0) & (lane < frame_dev - 1), usable, 0.0)
    number = mels * jnp.sum(inner, axis=1, keepdims=True)
    centre = jnp.sum(jnp.sum(x, axis=0, keepdims=True), axis=1, keepdims=True)
    centre = centre / (mels * jnp.maximum(jnp.sum(usable, axis=1, keepdims=True), 1.0))
    centre = lax.reduce_precision(centre, 8, 7)
    row = iota((mels, frame_dev), 0)

    def mel_shift(v, i):
        if i == 1:
            return v
        if i == 0:
            return jnp.where(row == 0, 0.0, pltpu.roll(v, 1, 0))
        return jnp.where(row == mels - 1, 0.0, pltpu.roll(v, mels - 1, 0))

    shifted = [pltpu.roll(x, 1, 1) * behind, x, pltpu.roll(x, frame_dev - 1, 1) * ahead]
    features = feature_rows(shifted, mel_shift, inner, centre)
    lane = iota((1, 128), 1)
    features = jnp.where(lane == 90, centre, jnp.where(lane == 91, number, features))
    high = lax.reduce_precision(features, 8, 7)
    mid = lax.reduce_precision(features - high, 8, 7)
    low = features - high - mid
    pick = iota((8, frame_dev), 0)
    column = jnp.where(pick < 4, pick, frame_dev - 8 + pick)
    edges = dot((iota((8, frame_dev), 1) == column).astype(BF16), x.astype(BF16), ((1,), (1,)))
    edges = jnp.concatenate([edges, jnp.zeros((8, 128 - mels), F32)], axis=1)
    target = iota((count, half), 0)
    at = iota((count, half), 1)
    choose = ((target == me_t - 1) & (at == 0)) | ((target == me_t + 1) & (at == half - 1))
    choose = choose.astype(BF16)
    above = recv[jnp.maximum(me_m - 1, 0), 2 * rows :]
    below = recv[jnp.minimum(me_m + 1, n_mel - 1), 2 * rows :]
    columns = dot(choose, own[...], ((1,), (1,)))
    outer = jnp.concatenate([dot(choose, above, ((1,), (1,))), dot(choose, below, ((1,), (1,)))], axis=1)
    parts = columns.shape[1] // 128
    for q in range(parts):
        spread[pl.ds(8 + q, count, stride=16), :] = columns[:, 128 * q : 128 * (q + 1)]
    spread[pl.ds(8 + parts, count, stride=16), :] = outer
    common = jnp.concatenate([high, mid, low], axis=0)
    for j in range(count):
        tail = jnp.concatenate([spread[16 * j + 8 : 16 * j + 13, :], common], axis=0)
        out[j] = jnp.concatenate([edges, tail], axis=0).astype(BF16)


def expand(recv_mel, recv_tm, own, out, temp):
    me_m, me_t = lax.axis_index("mel"), lax.axis_index("tm")
    n_mel, count = recv_mel.shape[0], recv_tm.shape[0]
    half = own.shape[1]
    rows = MEL_ROWS // 2
    chan = own.shape[0] // rows
    wide = out.shape[1]
    above = recv_mel[jnp.maximum(me_m - 1, 0), 2 * MEL_ROWS :]
    below = recv_mel[jnp.minimum(me_m + 1, n_mel - 1), 2 * MEL_ROWS :]
    every = jnp.concatenate([own[...], above, below], axis=0)
    after = recv_tm[jnp.minimum(me_t + 1, count - 1)].astype(F32)
    before = recv_tm[jnp.maximum(me_t - 1, 0)].astype(F32)
    after = jnp.concatenate([after[8 + q : 9 + q] for q in range(5)], axis=1)
    before = jnp.concatenate([before[8 + q : 9 + q] for q in range(5)], axis=1)
    side = iota((16, after.shape[1]), 0)
    sides = jnp.where(side == 0, after, jnp.where(side == 1, before, 0.0)).astype(BF16)
    lane = iota((half, wide), 1)
    spread = jnp.where((lane >> 1 == iota((half, wide), 0)) & (lane < 2 * half), 0.25, 0.0).astype(BF16)
    lane = iota((16, wide), 1)
    side = iota((16, wide), 0)
    right = (side == 0) & (lane >= 2 * half) & (lane < 2 * half + 2)
    left = (side == 1) & (lane >= wide - 2)
    columns = jnp.where(right | left, 0.25, 0.0).astype(BF16)
    full = dot(every, spread) + dot(sides, columns, ((0,), (0,)))
    for part in range(wide // 128):
        cut = slice(128 * part, 128 * (part + 1))
        temp[...] = full[: chan * rows, cut]
        for r in range(rows):
            out[(r + 1) * chan : (r + 2) * chan, cut] = temp[pl.ds(r, chan, stride=rows), :]
    out[0:chan] = full[chan * rows : chan * (rows + 1)]
    out[(rows + 1) * chan :] = full[chan * (rows + 1) :]


def silu_halves(h):
    t = jnp.tanh(h)
    one = 1.0 + t
    return h * one, one * (1.0 + h * (1.0 - t))


def forward_one(recv_mel, recv_tm, pairs, singles, twice, w1, wf, params, masks, edge_masks,
                pre_two, payload, own_act, x3, stats, features_out, act, pre_one, xs):
    n_mel, count = recv_mel.shape[0], recv_tm.shape[0]
    rows = MEL_ROWS
    mels = n_mel * rows
    half = recv_mel.shape[2]
    frame_dev = 2 * half
    wide = frame_dev + RIM
    chan = params.shape[1]
    me_m, me_t = lax.axis_index("mel"), lax.axis_index("tm")
    usable, behind, ahead = (masks[n : n + 1] for n in range(3))
    total = masks[3:4, 0:1]
    x = jnp.concatenate(
        [
            jnp.concatenate([recv_mel[j, 0:rows] for j in range(n_mel)], axis=0),
            jnp.concatenate([recv_mel[j, rows : 2 * rows] for j in range(n_mel)], axis=0),
        ],
        axis=1,
    ).astype(F32)
    after = recv_tm[jnp.minimum(me_t + 1, count - 1)].astype(F32)[0:8, :mels]
    before = recv_tm[jnp.maximum(me_t - 1, 0)].astype(F32)[0:8, :mels]
    after = jnp.where(me_t + 1 < count, after, 0.0)
    before = jnp.where(me_t > 0, before, 0.0)
    sides = jnp.concatenate([after[0:4], before[4:8], jnp.zeros((8, mels), F32)], axis=0).astype(BF16)
    side = iota((16, RIM), 0)
    place = iota((16, RIM), 1) == jnp.where(side < 4, side, jnp.where(side < 8, side + RIM - 8, -1))
    x = jnp.concatenate([x, dot(sides, place.astype(BF16), ((0,), (0,)))], axis=1) * usable
    xs[0:8] = jnp.zeros((8, wide), F32)
    xs[mels : mels + 8] = jnp.zeros((8, wide), F32)
    xs[4 : mels + 4] = x
    near = xs[pl.ds(pl.multiple_of(me_m * rows, 8), BAND), :]
    x3[...] = jnp.concatenate(
        [
            pltpu.roll(near, 1, 1) * behind,
            near,
            pltpu.roll(near, wide - 1, 1) * ahead,
            jnp.broadcast_to(usable, (BAND, wide)),
            jnp.zeros((128 - 4 * BAND, wide), F32),
        ],
        axis=0,
    ).astype(BF16)
    pre_one[...] = dot(w1[...], x3[...])
    parts = [recv_tm[d].astype(F32)[8:16] for d in range(count)]
    parts = [p[5:6] + p[6:7] + p[7:8] for p in parts]
    centres = [p[:, 90:91] for p in parts]
    numbers = [p[:, 91:92] for p in parts]
    weight = functools.reduce(jnp.add, numbers)
    centre = functools.reduce(jnp.add, [c * n for c, n in zip(centres, numbers)]) / jnp.maximum(weight, 1.0)
    lane = iota((1, 128), 1)
    features = jnp.zeros((1, 128), F32)
    moved = jnp.zeros((1, 128), F32)
    for part, c, n in zip(parts, centres, numbers):
        delta = c - centre
        moved = moved + delta * part
        features = features + part + delta * n * jnp.where(lane < 81, delta, 1.0)
    moved = dot(jnp.broadcast_to(moved, (8, 128)), twice[...], precision=EXACT)[0:1]
    features = features + moved
    edge = recv_tm[:, 0:8, :].astype(F32).reshape(count * 8, 128)
    q_usable, q_behind, q_ahead = (edge_masks[:, n : n + 1] for n in range(3))
    lane = iota((count * 8, 128), 1)

    def lane_shift(v, i):
        if i == 1:
            return v
        if i == 0:
            return jnp.where(lane < mels, pltpu.roll(v, 1, 1), 0.0)
        return pltpu.roll(v, 127, 1)

    shifted = [
        pltpu.roll(edge, 1, 0) * q_behind,
        edge,
        pltpu.roll(edge, count * 8 - 1, 0) * q_ahead,
    ]
    features = features + feature_rows(shifted, lane_shift, jnp.where(lane < mels, q_usable, 0.0), centre)
    features = jnp.where(iota((1, 128), 1) < 90, features, 0.0)
    features_out[...] = jnp.concatenate(
        [features, jnp.broadcast_to(centre, (1, 128)), jnp.zeros((6, 128), F32)], axis=0
    )
    near_mean = jnp.sum(singles[...] * features, axis=1, keepdims=True) / total
    square = jnp.sum(pairs[...] * features, axis=1, keepdims=True) / total
    inv = lax.rsqrt(square - near_mean * near_mean + 1e-05)
    mean = near_mean + centre * jnp.sum(singles[...], axis=1, keepdims=True)
    lane = iota((chan, 128), 1)
    stats[0:chan] = jnp.where(lane == 0, mean, jnp.where(lane == 1, inv, 0.0))
    stats[chan : chan + 8] = jnp.broadcast_to(to_lanes(near_mean), (8, 128))
    stats[chan + 8 : chan + 16] = jnp.broadcast_to(to_lanes(inv), (8, 128))
    scale = 0.5 * to_column(params[0:1], chan) * inv
    shift = 0.5 * to_column(params[1:2], chan) - mean * scale
    stats[chan + 16 :] = jnp.where(lane == 0, scale, jnp.where(lane == 1, shift, 0.0))
    scale = jnp.broadcast_to(scale, (chan, wide))
    shift = jnp.broadcast_to(shift, (chan, wide))
    ext = w1.shape[0] // chan
    block, taps = wf.shape
    first = jnp.zeros((chan, 128), F32)
    second = jnp.zeros((chan, 128), F32)
    own_mask = usable[:, :frame_dev]
    for r in range(ext):
        value, _ = silu_halves(pre_one[r * chan : (r + 1) * chan, :] * scale + shift)
        value = value * (usable * row_valid(r - 3, rows))
        base = r * 3 * chan
        low = value.astype(BF16)
        act[base : base + chan, :] = (pltpu.roll(value, 1, 1) * behind).astype(BF16)
        act[base + chan : base + 2 * chan, :] = low
        act[base + 2 * chan : base + 3 * chan, :] = (pltpu.roll(value, wide - 1, 1) * ahead).astype(BF16)
        if 2 <= r < rows + 4:
            own_act[(r - 2) * chan : (r - 1) * chan] = low[:, :frame_dev]
        if r < 5 or (r - 5) % 4:
            continue
        g = (r - 5) // 4
        result = dot(wf[...], act[g * 3 * block : g * 3 * block + taps, :])
        pre_two[g * block : (g + 1) * block] = result
        for q in range(4):
            if 2 <= 4 * g + q < rows + 2:
                p = result[q * chan : (q + 1) * chan, :frame_dev]
                masked = p * own_mask
                first = first + halves(masked)
                second = second + halves(masked * p)
    first = jnp.sum(first, axis=1, keepdims=True)
    second = jnp.sum(second, axis=1, keepdims=True)
    payload[...] = jnp.broadcast_to(to_lanes(first) + to_lanes(second, chan), payload.shape)


def backward_scaled(recv, pre_two, recv_mel, recv_tm, pooled_own, params, masks, grad, payload, pairs, stats, up, temp):
    expand(recv_mel, recv_tm, pooled_own, up, temp)
    chan = params.shape[1]
    rows = MEL_ROWS
    wide = pre_two.shape[1]
    frame_dev = wide - RIM
    usable = masks[0:1]
    total = masks[3:4, 0:1]
    sums = jnp.sum(recv[...], axis=0, keepdims=True)
    mean = to_column(sums, chan) / total
    inv = lax.rsqrt(to_column(sums, chan, chan) / total - mean * mean + 1e-05)
    lane = iota((chan, 128), 1)
    stats[...] = jnp.where(lane == 0, mean, jnp.where(lane == 1, inv, 0.0))
    mean = jnp.broadcast_to(mean, (chan, wide))
    inv = jnp.broadcast_to(inv, (chan, wide))
    scale = 0.5 * to_column(params[2:3], chan)
    shift = jnp.broadcast_to(0.5 * to_column(params[3:4], chan), (chan, wide))
    scale = jnp.broadcast_to(scale, (chan, wide))

    first = jnp.zeros((chan, 128), F32)
    second = jnp.zeros((chan, 128), F32)
    own_mask = usable[:, :frame_dev]
    for q in range(rows + 4):
        r = q // 2
        at = slice(q * chan, (q + 1) * chan)
        mask = usable * (0.5 * row_valid(q - 2, rows))
        normed = (pre_two[at, :] - mean) * inv
        value, slope = silu_halves(normed * scale + shift)
        g = up[r * chan : (r + 1) * chan, :] * slope * mask
        grad[at, :] = g
        if 2 <= q < rows + 2:
            g = g[:, :frame_dev]
            first = first + halves(g * normed[:, :frame_dev])
            second = second + halves(g)
            value = value[:, :frame_dev] * own_mask
            both = value if q % 2 == 0 else both + value
            if q % 2:
                pairs[(r - 1) * chan : r * chan, :] = both
    first = jnp.sum(first, axis=1, keepdims=True)
    second = jnp.sum(second, axis=1, keepdims=True)
    payload[...] = jnp.broadcast_to(to_lanes(first) + to_lanes(second, chan), payload.shape)


def pool(pairs, after, out, temp):
    del after
    chan, rows, half = out.shape[1:]
    to_mean = jnp.where(iota((2 * half, half), 0) >> 1 == iota((2 * half, half), 1), 0.25, 0.0)
    pooled = dot(pairs[...], to_mean, precision=EXACT)
    for r in range(rows):
        temp[pl.ds(r, chan, stride=rows), :] = pooled[r * chan : (r + 1) * chan]
    out[0] = temp[...].reshape(chan, rows, half).astype(BF16)


def backward_two(recv, pre_two, grad, stats, params, masks, act, out, payload, gain_out, bias_out, shifted):
    chan = params.shape[1]
    rows = MEL_ROWS
    wide = pre_two.shape[1]
    frame_dev = wide - RIM
    usable, behind, ahead = (masks[n : n + 1] for n in range(3))
    behind, ahead = behind[:, :frame_dev], ahead[:, :frame_dev]
    total = masks[3:4, 0:1]
    sums = jnp.sum(recv[...], axis=0, keepdims=True)
    gain_out[...] = sums[:, :chan]
    bias_out[...] = sums[:, chan:]
    mean, inv = stats[:, 0:1], stats[:, 1:2]
    factor = to_column(params[2:3], chan) * inv
    gain_part = jnp.broadcast_to(to_column(sums, chan) / total * inv, (chan, wide))
    bias_part = jnp.broadcast_to(to_column(sums, chan, chan) / total, (chan, wide))
    mean = jnp.broadcast_to(mean, (chan, wide))
    factor = jnp.broadcast_to(factor, (chan, wide))
    count = pre_two.shape[0] // chan

    table = jnp.zeros((3 * chan, 3 * chan), F32)
    for q in range(count):
        at = slice(q * chan, (q + 1) * chan)
        mask = usable * row_valid(q - 2, rows)
        centred = grad[at, :] - (bias_part + (pre_two[at, :] - mean) * gain_part) * mask
        value = factor * centred
        low = value.astype(BF16)
        out[at, :] = low
        m = q - 2
        if not 0 <= m < rows:
            continue
        base = m * 3 * chan
        shifted[base : base + chan, :] = (pltpu.roll(value, 1, 1)[:, :frame_dev] * behind).astype(BF16)
        shifted[base + chan : base + 2 * chan, :] = low[:, :frame_dev]
        shifted[base + 2 * chan : base + 3 * chan, :] = (
            pltpu.roll(value, wide - 1, 1)[:, :frame_dev] * ahead
        ).astype(BF16)
        if m % 4 == 3:
            four = range(m - 3, m + 1)
            left = jnp.concatenate([shifted[n * 3 * chan : (n + 1) * 3 * chan, :] for n in four], axis=1)
            right = jnp.concatenate([act[n * chan : (n + 3) * chan, :] for n in four], axis=1)
            table = table + dot(left, right, ((1,), (1,)))
    payload[0 : 3 * chan] = table[:, :128]
    upper = 3 * chan // 2
    payload[3 * chan :] = jnp.concatenate([table[:upper, 128:], table[upper:, 128:]], axis=1)


def backward_one(grad, w1, x3, stats, masks, wb_hbm, g1, sums, g3, pre_one, wb, sem):
    fetch = pltpu.make_async_copy(wb_hbm, wb, sem)
    fetch.start()
    chan = wb.shape[0] // 4
    rows = MEL_ROWS
    wide = x3.shape[1]
    frame_dev = wide - RIM
    usable, behind, ahead = (masks[n : n + 1] for n in range(3))
    block = wb.shape[0]
    count = grad.shape[0] // chan
    pre_one[...] = dot(w1[2 * chan : (rows + 4) * chan], x3[...])

    scale = jnp.broadcast_to(stats[chan + 16 :, 0:1], (chan, wide))
    shift = jnp.broadcast_to(stats[chan + 16 :, 1:2], (chan, wide))
    fetch.wait()
    for q in range(count):
        low = grad[q * chan : (q + 1) * chan, :]
        value = low.astype(F32)
        base = q * 3 * chan
        g3[base : base + chan, :] = (pltpu.roll(value, 1, 1) * behind).astype(BF16)
        g3[base + chan : base + 2 * chan, :] = low
        g3[base + 2 * chan : base + 3 * chan, :] = (pltpu.roll(value, wide - 1, 1) * ahead).astype(BF16)
        if q < count - 1 and (q < 5 or (q - 5) % 4):
            continue
        start = 4 * ((q - 2) // 4)
        step = min(4, rows + 2 - start)
        result = dot(
            wb[: step * chan, : (step + 2) * 3 * chan], g3[start * 3 * chan : (start + step + 2) * 3 * chan, :]
        )
        for n in range(step):
            at = slice((start + n) * chan, (start + n + 1) * chan)
            _, slope = silu_halves(pre_one[at, :] * scale + shift)
            mask = usable * (0.5 * row_valid(start + n - 1, rows))
            g1[at, :] = result[n * chan : (n + 1) * chan] * slope * mask
    table = jnp.zeros((chan, 128), F32)
    for g in range(rows // 4):
        part = g1[chan + g * block : chan + (g + 1) * block, :frame_dev]
        high = lax.reduce_precision(part, 8, 7)
        low = (part - high).astype(BF16)
        taps_in = x3[:, :frame_dev]
        products = dot(high.astype(BF16), taps_in, ((1,), (1,))) + dot(low, taps_in, ((1,), (1,)))
        for m in range(4):
            table = table + pltpu.roll(products[m * chan : (m + 1) * chan], 128 - (4 * g + m + 3), 1)
    tap = iota((16, 128), 0)
    lane = iota((16, 128), 1)
    i = (tap * 11) >> 5
    select = ((lane == BAND * (tap - 3 * i) + i) & (tap < 9)) | ((lane == 3 * BAND) & (tap == 9))
    rows10 = dot(select.astype(F32), table, ((1,), (1,)), EXACT)
    sums[...] = jnp.concatenate(
        [jnp.concatenate([rows10[0:5], rows10[5:10]], axis=1), jnp.zeros((3, 128), F32)], axis=0
    )


def collect(recv, sums, out):
    count = out.shape[0] // 14
    share = recv.shape[0] // count
    mine = recv[0:share, :]
    for d in range(1, count):
        mine = mine + recv[share * d : share * (d + 1), :]
    block = jnp.concatenate([sums[0:5], mine] + [jnp.zeros((9 - share, 128), F32)] * (share < 9), axis=0)
    for d in range(count):
        out[14 * d : 14 * (d + 1), :] = block


def finish(recv, features, stats, k1t, g1, w1, x3, params, masks, ws_hbm,
           spec_grad, kernel_one, kernel_two, gain_out, bias_out, low, taps_out, table, pre_one, ws, sem):
    fetch = pltpu.make_async_copy(ws_hbm, ws, sem)
    fetch.start()
    chan = params.shape[1]
    rows = MEL_ROWS
    wide = g1.shape[1]
    frame_dev = wide - RIM
    usable, behind, ahead = (masks[n : n + 1] for n in range(3))
    total = masks[3:4, 0:1]
    gain = params[0:1]
    count = recv.shape[0] // 14
    share = -(-9 * chan * chan // 128 // count)
    sums = recv[0:5, :]
    for d in range(1, count):
        sums = sums + recv[14 * d : 14 * d + 5, :]
    ten = jnp.concatenate([sums[:, :chan], sums[:, chan:]], axis=0)
    bias_sum = ten[9:10]
    mean_l, inv_l = stats[chan : chan + 1, :chan], stats[chan + 8 : chan + 9, :chan]
    pre_one[...] = dot(w1[2 * chan : (rows + 4) * chan], x3[...])
    ten = ten - features[1:2, 0:1] * bias_sum
    k = k1t[0:9]
    gain_sum = inv_l * (jnp.sum(k * ten[0:9], axis=0, keepdims=True) - mean_l * bias_sum)
    gain_out[...] = gain_sum
    bias_out[...] = bias_sum
    row = features[0:1, :]
    lane = iota((1, 128), 1)
    gram = jnp.concatenate(
        [jnp.where(lane < 9, pltpu.roll(row, 128 - 9 * t, 1) if t else row, 0.0) for t in range(9)]
        + [jnp.zeros((7, 128), F32)],
        axis=0,
    )
    single = to_column(row, 16, 81)[0:9]
    k_rows = jnp.concatenate([k1t[...], jnp.zeros((112, chan), F32)], axis=0)
    normed_taps = inv_l * (dot(gram, k_rows, precision=EXACT)[0:9] - single * mean_l)
    factor_l = gain * inv_l
    grad_taps = factor_l * (ten[0:9] - (bias_sum * single + gain_sum * normed_taps) / total)
    for i in range(3):
        kernel_one[i] = grad_taps[3 * i : 3 * i + 3]
    mean, inv = stats[0:chan, 0:1], stats[0:chan, 1:2]
    factor = jnp.broadcast_to(to_column(gain, chan) * inv, (chan, wide))
    gain_part = jnp.broadcast_to(to_column(gain_sum, chan) / total * inv, (chan, wide))
    bias_part = jnp.broadcast_to(to_column(bias_sum, chan) / total, (chan, wide))
    mean = jnp.broadcast_to(mean, (chan, wide))

    for q in range(rows + 2):
        at = slice(q * chan, (q + 1) * chan)
        mask = usable * row_valid(q - 1, rows)
        centred = g1[at, :] - (bias_part + (pre_one[at, :] - mean) * gain_part) * mask
        low[at, :] = (factor * centred).astype(BF16)
    fetch.wait()
    taps_out[...] = dot(ws[...], low[...])
    for part in range(3):
        cut = slice(128 * part, 128 * (part + 1))
        table[part] = taps_out[:, cut]
    moved = [
        jnp.concatenate([table[part, pl.ds(b, rows, stride=8), :] for part in range(3)], axis=1) for b in range(3)
    ]
    result = pltpu.roll(moved[0], 1, 1) * behind + moved[1] + pltpu.roll(moved[2], wide - 1, 1) * ahead
    spec_grad[0] = (result * usable)[:, :frame_dev]
    whole = jnp.concatenate([recv[14 * d + 5 : 14 * d + 5 + share, :] for d in range(count)], axis=0)
    upper = 3 * chan // 2
    main = whole[: 3 * chan]
    rest = whole[3 * chan : 3 * chan + upper]
    last = jnp.concatenate([rest[:, :chan], rest[:, chan:]], axis=0)
    for j in range(3):
        at = slice((2 - j) * chan, (3 - j) * chan)
        kernel_two[j] = main[at, :chan]
        kernel_two[3 + j] = main[at, chan:]
        kernel_two[6 + j] = last[at]


def run(kernel, outs, scratch, *args, hbm=0, apart=(), flops=10**8, size=4 * 10**6):
    vmem = pl.BlockSpec(memory_space=pltpu.VMEM)
    specs = []
    args = list(args)
    for n, a in enumerate(args):
        if hbm and n >= len(args) - hbm:
            specs.append(pl.BlockSpec(memory_space=pltpu.HBM))
            args[n] = pltpu.with_memory_space_constraint(a, pltpu.HBM)
        else:
            specs.append(vmem)
            args[n] = pltpu.with_memory_space_constraint(a, pltpu.VMEM)
    return pl.pallas_call(
        kernel,
        out_shape=outs,
        in_specs=specs,
        out_specs=[pl.BlockSpec(memory_space=pltpu.HBM) if n in apart else vmem for n in range(len(outs))],
        scratch_shapes=scratch,
        compiler_params=pltpu.CompilerParams(vmem_limit_bytes=30 * 2**20),
        cost_estimate=pl.CostEstimate(flops=flops, bytes_accessed=size, transcendentals=0),
    )(*args)


def shape(dims, dtype=F32):
    return jax.ShapeDtypeStruct(dims, dtype)


def kept(dims, dtype=F32):
    return pltpu.VMEM(dims, dtype)


def exchange(blocks, axes=AXES):
    return lax.all_to_all(blocks, axes, 0, 0, tiled=True)


def exchange_rows(rows, axes=AXES):
    return exchange(rows[:, None, :], axes)[:, 0, :]


def shards(spectrum, clip_bounds, kernel_one, gain_one, bias_one, kernel_two, gain_two, bias_two, pooled_grad):
    _, rows, frame_dev = spectrum.shape
    chan = kernel_two.shape[0]
    n_mel, n_tm = lax.axis_size("mel"), lax.axis_size("tm")
    devices = n_mel * n_tm
    half = frame_dev // 2
    wide = frame_dev + RIM
    mels = n_mel * rows

    packed, own = run(
        pack_mel,
        [kept((n_mel, 2 * rows + chan, half), BF16), kept((chan * rows // 2, half), BF16)],
        [
            pltpu.VMEM(spectrum.shape, BF16),
            pltpu.VMEM(pooled_grad.shape, BF16),
            pltpu.SemaphoreType.DMA((2,)),
        ],
        spectrum,
        pooled_grad,
        hbm=2,
    )
    recv_mel = exchange(packed, "mel")
    ext = rows + 6
    span = 6 * 3 * chan
    wf, wb, w1, ws, pairs, singles, k1t, params, masks, edge_masks, twice = run(
        weights,
        [
            kept((4 * chan, span), BF16),
            shape((4 * chan, span), BF16),
            kept((ext * chan, 128), BF16),
            shape((rows * 8, (rows + 2) * chan), BF16),
            kept((chan, 128)),
            kept((chan, 128)),
            kept((16, chan)),
            kept((8, chan)),
            kept((8, wide)),
            kept((n_tm * 8, 128)),
            kept((128, 128)),
        ],
        [
            pltpu.VMEM((9, chan, chan), BF16),
            pltpu.VMEM((3, 3, chan), BF16),
            pltpu.VMEM((4, 1, chan), F32),
            pltpu.SMEM(clip_bounds.shape, jnp.int32),
            pltpu.VMEM((4 * chan, span), BF16),
            pltpu.VMEM((rows * 8, (rows + 2) * chan), BF16),
            pltpu.SemaphoreType.DMA((9,)),
        ],
        clip_bounds,
        jnp.transpose(kernel_two, (2, 3, 0, 1)).reshape(9, chan, chan),
        jnp.transpose(kernel_one, (1, 2, 0)),
        gain_one[None],
        bias_one[None],
        gain_two[None],
        bias_two[None],
        hbm=7,
        apart=(1, 3),
    )
    (packed,) = run(
        pack_tm,
        [kept((n_tm, 16, 128), BF16)],
        [pltpu.VMEM((n_tm * 16, 128), F32)],
        recv_mel,
        own,
        masks,
    )
    recv_tm = exchange(packed, "tm")
    pre_two, payload, act, x3, stats_one, features = run(
        forward_one,
        [
            kept(((rows + 4) * chan, wide)),
            kept((devices, 128)),
            kept(((rows + 2) * chan, frame_dev), BF16),
            kept((128, wide), BF16),
            kept((2 * chan + 16, 128)),
            kept((8, 128)),
        ],
        [
            pltpu.VMEM((ext * 3 * chan, wide), BF16),
            pltpu.VMEM((ext * chan, wide), F32),
            pltpu.VMEM((mels + 8, wide), F32),
        ],
        recv_mel,
        recv_tm,
        pairs,
        singles,
        twice,
        w1,
        wf,
        params,
        masks,
        edge_masks,
    )
    recv = exchange_rows(payload)
    grad, payload, row_pairs, stats_two = run(
        backward_scaled,
        [
            kept(((rows + 4) * chan, wide)),
            kept((devices, 128)),
            kept((rows // 2 * chan, frame_dev)),
            kept((chan, 128)),
        ],
        [pltpu.VMEM(((rows // 2 + 2) * chan, wide), F32), pltpu.VMEM((rows // 2 * chan, 128), F32)],
        recv,
        pre_two,
        recv_mel,
        recv_tm,
        own,
        params,
        masks,
    )
    recv = exchange_rows(payload)
    pieces = 9 * chan * chan // 128
    grad, payload, gain_two_grad, bias_two_grad = run(
        backward_two,
        [kept(((rows + 4) * chan, wide), BF16), kept((pieces, 128)), shape((1, chan)), shape((1, chan))],
        [pltpu.VMEM((rows * 3 * chan, frame_dev), BF16)],
        recv,
        pre_two,
        grad,
        stats_two,
        params,
        masks,
        act,
    )
    share = -(-pieces // devices)
    if share * devices > pieces:
        payload = jnp.pad(payload, ((0, share * devices - pieces), (0, 0)))
    recv = exchange_rows(payload)
    g1, sums = run(
        backward_one,
        [kept(((rows + 2) * chan, wide)), kept((8, 128))],
        [
            pltpu.VMEM(((rows + 4) * 3 * chan, wide), BF16),
            pltpu.VMEM(((rows + 2) * chan, wide), F32),
            pltpu.VMEM((4 * chan, span), BF16),
            pltpu.SemaphoreType.DMA,
        ],
        grad,
        w1,
        x3,
        stats_one,
        masks,
        wb,
        hbm=1,
    )
    (payload,) = run(collect, [kept((devices * 14, 128))], [], recv, sums)
    recv = exchange_rows(payload)
    (pooled,) = run(
        pool,
        [shape((1, chan, rows // 2, half), BF16)],
        [pltpu.VMEM((rows // 2 * chan, 128), F32)],
        row_pairs,
        sums,
    )
    spec_grad, kernel_one_grad, kernel_two_grad, gain_one_grad, bias_one_grad = run(
        finish,
        [
            shape((1, rows, frame_dev)),
            shape((3, 3, chan)),
            shape((9, chan, chan)),
            shape((1, chan)),
            shape((1, chan)),
        ],
        [
            pltpu.VMEM(((rows + 2) * chan, wide), BF16),
            pltpu.VMEM((rows * 8, wide), F32),
            pltpu.VMEM((3, rows * 8, 128), F32),
            pltpu.VMEM(((rows + 2) * chan, wide), F32),
            pltpu.VMEM((rows * 8, (rows + 2) * chan), BF16),
            pltpu.SemaphoreType.DMA,
        ],
        recv,
        features,
        stats_one,
        k1t,
        g1,
        w1,
        x3,
        params,
        masks,
        ws,
        hbm=1,
    )
    kernel_two_grad = jnp.transpose(kernel_two_grad.reshape(3, 3, chan, chan), (2, 3, 0, 1))
    return (
        pooled,
        spec_grad,
        jnp.transpose(kernel_one_grad, (2, 0, 1)),
        gain_one_grad[0],
        bias_one_grad[0],
        kernel_two_grad,
        gain_two_grad[0],
        bias_two_grad[0],
    )


def solution(mesh):
    return jax.shard_map(
        shards,
        mesh=mesh,
        in_specs=(
            P(None, "mel", "tm"),
            P(),
            P(),
            P(),
            P(),
            P(),
            P(),
            P(),
            P(None, None, "mel", "tm"),
        ),
        out_specs=(P(None, None, "mel", "tm"), P(None, "mel", "tm"), P(), P(), P(), P(), P(), P()),
        check_vma=False,
    )
```

```python
import functools

import jax
import jax.numpy as jnp
from jax import lax
from jax.experimental import pallas as pl
from jax.experimental.pallas import tpu as pltpu
from jax.sharding import PartitionSpec as P

F32 = jnp.float32
BF16 = jnp.bfloat16
AXES = ("mel", "tm")
EXACT = lax.Precision.HIGHEST
RIM = 128
BAND = 24
MEL_ROWS = 16


def iota(shape, dim):
    return lax.broadcasted_iota(jnp.int32, shape, dim)


def dot(a, b, over=((1,), (0,)), precision=None):
    return lax.dot_general(a, b, (over, ((), ())), precision=precision, preferred_element_type=F32)


def to_column(lanes, count, start=0):
    shape = (count, lanes.shape[1])
    return jnp.sum(jnp.where(iota(shape, 1) == iota(shape, 0) + start, lanes, 0.0), axis=1, keepdims=True)


def to_lanes(column, start=0, width=128):
    shape = (column.shape[0], width)
    return jnp.sum(jnp.where(iota(shape, 1) == iota(shape, 0) + start, column, 0.0), axis=0, keepdims=True)


def halves(v):
    return sum(v[:, n : n + 128] for n in range(128, v.shape[1], 128)) + v[:, :128]


def frame_masks(bounds, frames):
    last = bounds.shape[1] - 1

    def living(f):
        return (f >= 0) & (f < bounds[0, last])

    def paired(f):
        both = living(f) & living(f + 1)
        for k in range(1, last):
            both = both & (f + 1 != bounds[0, k])
        return both

    return tuple(m.astype(F32) for m in (living(frames), paired(frames - 1), paired(frames)))


def row_valid(row, rows):
    mel = lax.axis_index("mel") * rows + row
    return ((mel >= 0) & (mel < lax.axis_size("mel") * rows)).astype(F32)


def load_all(*pairs, sems):
    copies = [pltpu.make_async_copy(src, dst, sems.at[n]) for n, (src, dst) in enumerate(pairs)]
    for copy in copies:
        copy.start()
    for copy in copies:
        copy.wait()


def pack_mel(spec_hbm, grad_hbm, out, own, spec, sems):
    load_all((spec_hbm, spec), (grad_hbm, own), sems=sems)
    me = lax.axis_index("mel")
    x = spec[0]
    rows, frame_dev = x.shape
    half = frame_dev // 2
    g = own[0].astype(F32)
    top = g[:, 0, :]
    bottom = g[:, g.shape[1] - 1, :]
    for j in range(out.shape[0]):
        out[j, 0:rows] = x[:, :half]
        out[j, rows : 2 * rows] = x[:, half:]
        edge = jnp.where(j == me - 1, top, 0.0) + jnp.where(j == me + 1, bottom, 0.0)
        out[j, 2 * rows :] = edge.astype(BF16)


def weights(bounds_hbm, k2_hbm, k1_hbm, gain_one_hbm, bias_one_hbm, gain_two_hbm, bias_two_hbm,
            wf, wb_hbm, w1, ws_hbm, pairs, singles, k1t, params, masks, edge_masks, twice,
            k2, k1, vectors, bounds, wb, ws, sems):
    load_all(
        (bounds_hbm, bounds),
        (k2_hbm, k2),
        (k1_hbm, k1),
        (gain_one_hbm, vectors.at[0]),
        (bias_one_hbm, vectors.at[1]),
        (gain_two_hbm, vectors.at[2]),
        (bias_two_hbm, vectors.at[3]),
        sems=sems,
    )
    chan = k2.shape[1]
    span = wf.shape[1]
    wide = masks.shape[1]
    frame_dev = wide - RIM
    lane = iota((1, wide), 1)
    frames = lax.axis_index("tm") * frame_dev + jnp.where(lane < frame_dev + RIM // 2, lane, lane - wide)
    last = bounds.shape[1] - 1
    pixels = (bounds[0, last] * (lax.axis_size("mel") * MEL_ROWS)).astype(F32)
    masks[...] = jnp.concatenate(
        list(frame_masks(bounds, frames)) + [jnp.full((1, wide), 1.0) * pixels, jnp.zeros((4, wide), F32)], axis=0
    )
    q = iota(edge_masks.shape, 0)
    lane = iota(edge_masks.shape, 1)
    k = q % 8
    frames = (q // 8) * frame_dev + jnp.where(k < 4, k, k + frame_dev - 8)
    living, behind, ahead = frame_masks(bounds, frames)
    living = jnp.where((k == 0) | (k == 7), living, 0.0)
    edge_masks[...] = jnp.where(lane == 0, living, jnp.where(lane == 1, behind, jnp.where(lane == 2, ahead, 0.0)))
    params[...] = jnp.concatenate(
        [vectors[n] for n in range(4)] + [jnp.zeros((4, chan), F32)], axis=0
    )
    tap = iota((16, 128), 0)
    lane = iota((16, 128), 1)
    i = (tap * 11) >> 5
    ninth = (lane * 57) >> 9
    to_band = (lane == BAND * (tap - 3 * i) + i) & (tap < 9)
    to_left = (ninth == tap) & (tap < 9)
    to_right = (lane - 9 * ninth == tap) & (lane < 81)
    to_single = (lane == 81 + tap) & (tap < 9)
    source = iota((128, 128), 0) - 81
    lane = iota((128, 128), 1)
    ninth = (lane * 57) >> 9
    inside = (source >= 0) & (source < 9) & (lane < 81)
    twice[...] = jnp.where(inside, (source == ninth).astype(F32) + (source == lane - 9 * ninth).astype(F32), 0.0)
    taps = [k2[t].astype(F32) for t in range(9)]
    rest = jnp.zeros((chan, span - 9 * chan), F32)
    forward = jnp.concatenate(taps + [rest], axis=1)
    backward = jnp.concatenate([taps[8 - t].T for t in range(9)] + [rest], axis=1)
    for r in range(wb.shape[0] // chan):
        at = slice(r * chan, (r + 1) * chan)
        wb[at] = (pltpu.roll(backward, 3 * chan * r, 1) if r else backward).astype(BF16)
    store_wb = pltpu.make_async_copy(wb, wb_hbm, sems.at[7])
    store_wb.start()
    for r in range(wf.shape[0] // chan):
        at = slice(r * chan, (r + 1) * chan)
        wf[at] = (pltpu.roll(forward, 3 * chan * r, 1) if r else forward).astype(BF16)
    full = jnp.concatenate([k1[n].astype(F32) for n in range(3)] + [jnp.zeros((7, chan), F32)], axis=0)
    k1t[...] = full
    k = full.astype(BF16)
    lanes = [dot(k, select.astype(BF16), ((0,), (0,))) for select in (to_band, to_left, to_right, to_single)]
    pairs[...] = lanes[1] * lanes[2]
    singles[...] = lanes[3]
    for m in range(w1.shape[0] // chan):
        w1[m * chan : (m + 1) * chan] = (pltpu.roll(lanes[0], m, 1) if m else lanes[0]).astype(BF16)
    low = [
        jnp.concatenate([full[3 * (2 - a) + 2 - b : 3 * (2 - a) + 3 - b] for a in range(3)], axis=1)
        for b in range(3)
    ]
    base = jnp.concatenate(low + [jnp.zeros((5, 3 * chan), F32)], axis=0)
    base = jnp.concatenate([base, jnp.zeros((8, ws.shape[1] - 3 * chan), F32)], axis=1)
    for m in range(ws.shape[0] // 8):
        ws[8 * m : 8 * m + 8] = (pltpu.roll(base, chan * m, 1) if m else base).astype(BF16)
    store_ws = pltpu.make_async_copy(ws, ws_hbm, sems.at[8])
    store_ws.start()
    store_wb.wait()
    store_ws.wait()


def feature_rows(shifted, axis_shift, weight, centre):
    z = [None] * 9
    for j in range(3):
        for i in range(3):
            z[3 * i + j] = axis_shift(shifted[j], i) - centre

    def folded(v):
        if v.shape[1] > 128:
            v = v[:, :128] + v[:, 128:]
        return jnp.sum(v, axis=0, keepdims=True)

    rows = [None] * 96
    for s in range(9):
        left = z[s] * weight
        rows[81 + s] = folded(left)
        for t in range(s, 9):
            rows[9 * s + t] = rows[9 * t + s] = folded(left * z[t])
    zero = jnp.zeros((1, 128), F32)
    stack = jnp.concatenate([zero if r is None else r for r in rows], axis=0)
    return to_lanes(jnp.sum(stack, axis=1, keepdims=True))


def flat_rows(own):
    _, chan, rows, half = own.shape
    return own[0].astype(F32).reshape(chan * rows, half).astype(BF16)


def pack_tm(recv, own, masks, out, spread):
    count = out.shape[0]
    n_mel = recv.shape[0]
    me_m, me_t = lax.axis_index("mel"), lax.axis_index("tm")
    rows = MEL_ROWS
    half = recv.shape[2]
    frame_dev = 2 * half
    mels = n_mel * rows
    lane = iota((1, frame_dev), 1)
    usable, behind, ahead = (masks[n : n + 1, :frame_dev] for n in range(3))
    x = jnp.concatenate(
        [
            jnp.concatenate([recv[j, 0:rows] for j in range(n_mel)], axis=0),
            jnp.concatenate([recv[j, rows : 2 * rows] for j in range(n_mel)], axis=0),
        ],
        axis=1,
    )
    x = x.astype(F32) * usable
    inner = jnp.where((lane > 0) & (lane < frame_dev - 1), usable, 0.0)
    number = mels * jnp.sum(inner, axis=1, keepdims=True)
    centre = jnp.sum(jnp.sum(x, axis=0, keepdims=True), axis=1, keepdims=True)
    centre = centre / (mels * jnp.maximum(jnp.sum(usable, axis=1, keepdims=True), 1.0))
    centre = lax.reduce_precision(centre, 8, 7)
    row = iota((mels, frame_dev), 0)

    def mel_shift(v, i):
        if i == 1:
            return v
        if i == 0:
            return jnp.where(row == 0, 0.0, pltpu.roll(v, 1, 0))
        return jnp.where(row == mels - 1, 0.0, pltpu.roll(v, mels - 1, 0))

    shifted = [pltpu.roll(x, 1, 1) * behind, x, pltpu.roll(x, frame_dev - 1, 1) * ahead]
    features = feature_rows(shifted, mel_shift, inner, centre)
    lane = iota((1, 128), 1)
    features = jnp.where(lane == 90, centre, jnp.where(lane == 91, number, features))
    high = lax.reduce_precision(features, 8, 7)
    mid = lax.reduce_precision(features - high, 8, 7)
    low = features - high - mid
    pick = iota((8, frame_dev), 0)
    column = jnp.where(pick < 4, pick, frame_dev - 8 + pick)
    edges = dot((iota((8, frame_dev), 1) == column).astype(BF16), x.astype(BF16), ((1,), (1,)))
    edges = jnp.concatenate([edges, jnp.zeros((8, 128 - mels), F32)], axis=1)
    target = iota((count, half), 0)
    at = iota((count, half), 1)
    choose = ((target == me_t - 1) & (at == 0)) | ((target == me_t + 1) & (at == half - 1))
    choose = choose.astype(BF16)
    above = recv[jnp.maximum(me_m - 1, 0), 2 * rows :]
    below = recv[jnp.minimum(me_m + 1, n_mel - 1), 2 * rows :]
    columns = dot(choose, flat_rows(own), ((1,), (1,)))
    outer = jnp.concatenate([dot(choose, above, ((1,), (1,))), dot(choose, below, ((1,), (1,)))], axis=1)
    parts = columns.shape[1] // 128
    for q in range(parts):
        spread[pl.ds(8 + q, count, stride=16), :] = columns[:, 128 * q : 128 * (q + 1)]
    spread[pl.ds(8 + parts, count, stride=16), :] = outer
    common = jnp.concatenate([high, mid, low], axis=0)
    for j in range(count):
        tail = jnp.concatenate([spread[16 * j + 8 : 16 * j + 13, :], common], axis=0)
        out[j] = jnp.concatenate([edges, tail], axis=0).astype(BF16)


def expand(recv_mel, recv_tm, own, out, temp):
    me_m, me_t = lax.axis_index("mel"), lax.axis_index("tm")
    n_mel, count = recv_mel.shape[0], recv_tm.shape[0]
    chan, rows, half = own.shape[1:]
    wide = out.shape[1]
    above = recv_mel[jnp.maximum(me_m - 1, 0), 2 * MEL_ROWS :]
    below = recv_mel[jnp.minimum(me_m + 1, n_mel - 1), 2 * MEL_ROWS :]
    every = jnp.concatenate([flat_rows(own), above, below], axis=0)
    after = recv_tm[jnp.minimum(me_t + 1, count - 1)].astype(F32)
    before = recv_tm[jnp.maximum(me_t - 1, 0)].astype(F32)
    after = jnp.concatenate([after[8 + q : 9 + q] for q in range(5)], axis=1)
    before = jnp.concatenate([before[8 + q : 9 + q] for q in range(5)], axis=1)
    side = iota((16, after.shape[1]), 0)
    sides = jnp.where(side == 0, after, jnp.where(side == 1, before, 0.0)).astype(BF16)
    lane = iota((half, wide), 1)
    spread = jnp.where((lane >> 1 == iota((half, wide), 0)) & (lane < 2 * half), 0.25, 0.0).astype(BF16)
    lane = iota((16, wide), 1)
    side = iota((16, wide), 0)
    right = (side == 0) & (lane >= 2 * half) & (lane < 2 * half + 2)
    left = (side == 1) & (lane >= wide - 2)
    columns = jnp.where(right | left, 0.25, 0.0).astype(BF16)
    full = dot(every, spread) + dot(sides, columns, ((0,), (0,)))
    for part in range(wide // 128):
        cut = slice(128 * part, 128 * (part + 1))
        temp[...] = full[: chan * rows, cut]
        for r in range(rows):
            out[(r + 1) * chan : (r + 2) * chan, cut] = temp[pl.ds(r, chan, stride=rows), :]
    out[0:chan] = full[chan * rows : chan * (rows + 1)]
    out[(rows + 1) * chan :] = full[chan * (rows + 1) :]


def silu_halves(h):
    t = jnp.tanh(h)
    one = 1.0 + t
    return h * one, one * (1.0 + h * (1.0 - t))


def forward_one(recv_mel, recv_tm, pairs, singles, twice, w1, wf, params, masks, edge_masks,
                pre_two, payload, own_act, x3, stats, features_out, act, pre_one, xs):
    n_mel, count = recv_mel.shape[0], recv_tm.shape[0]
    rows = MEL_ROWS
    mels = n_mel * rows
    half = recv_mel.shape[2]
    frame_dev = 2 * half
    wide = frame_dev + RIM
    chan = params.shape[1]
    me_m, me_t = lax.axis_index("mel"), lax.axis_index("tm")
    usable, behind, ahead = (masks[n : n + 1] for n in range(3))
    total = masks[3:4, 0:1]
    x = jnp.concatenate(
        [
            jnp.concatenate([recv_mel[j, 0:rows] for j in range(n_mel)], axis=0),
            jnp.concatenate([recv_mel[j, rows : 2 * rows] for j in range(n_mel)], axis=0),
        ],
        axis=1,
    ).astype(F32)
    after = recv_tm[jnp.minimum(me_t + 1, count - 1)].astype(F32)[0:8, :mels]
    before = recv_tm[jnp.maximum(me_t - 1, 0)].astype(F32)[0:8, :mels]
    after = jnp.where(me_t + 1 < count, after, 0.0)
    before = jnp.where(me_t > 0, before, 0.0)
    sides = jnp.concatenate([after[0:4], before[4:8], jnp.zeros((8, mels), F32)], axis=0).astype(BF16)
    side = iota((16, RIM), 0)
    place = iota((16, RIM), 1) == jnp.where(side < 4, side, jnp.where(side < 8, side + RIM - 8, -1))
    x = jnp.concatenate([x, dot(sides, place.astype(BF16), ((0,), (0,)))], axis=1) * usable
    xs[0:8] = jnp.zeros((8, wide), F32)
    xs[mels : mels + 8] = jnp.zeros((8, wide), F32)
    xs[4 : mels + 4] = x
    near = xs[pl.ds(pl.multiple_of(me_m * rows, 8), BAND), :]
    x3[...] = jnp.concatenate(
        [
            pltpu.roll(near, 1, 1) * behind,
            near,
            pltpu.roll(near, wide - 1, 1) * ahead,
            jnp.broadcast_to(usable, (BAND, wide)),
            jnp.zeros((128 - 4 * BAND, wide), F32),
        ],
        axis=0,
    ).astype(BF16)
    pre_one[...] = dot(w1[...], x3[...])
    parts = [recv_tm[d].astype(F32)[8:16] for d in range(count)]
    parts = [p[5:6] + p[6:7] + p[7:8] for p in parts]
    centres = [p[:, 90:91] for p in parts]
    numbers = [p[:, 91:92] for p in parts]
    weight = functools.reduce(jnp.add, numbers)
    centre = functools.reduce(jnp.add, [c * n for c, n in zip(centres, numbers)]) / jnp.maximum(weight, 1.0)
    lane = iota((1, 128), 1)
    features = jnp.zeros((1, 128), F32)
    moved = jnp.zeros((1, 128), F32)
    for part, c, n in zip(parts, centres, numbers):
        delta = c - centre
        moved = moved + delta * part
        features = features + part + delta * n * jnp.where(lane < 81, delta, 1.0)
    moved = dot(jnp.broadcast_to(moved, (8, 128)), twice[...], precision=EXACT)[0:1]
    features = features + moved
    edge = recv_tm[:, 0:8, :].astype(F32).reshape(count * 8, 128)
    q_usable, q_behind, q_ahead = (edge_masks[:, n : n + 1] for n in range(3))
    lane = iota((count * 8, 128), 1)

    def lane_shift(v, i):
        if i == 1:
            return v
        if i == 0:
            return jnp.where(lane < mels, pltpu.roll(v, 1, 1), 0.0)
        return pltpu.roll(v, 127, 1)

    shifted = [
        pltpu.roll(edge, 1, 0) * q_behind,
        edge,
        pltpu.roll(edge, count * 8 - 1, 0) * q_ahead,
    ]
    features = features + feature_rows(shifted, lane_shift, jnp.where(lane < mels, q_usable, 0.0), centre)
    features = jnp.where(iota((1, 128), 1) < 90, features, 0.0)
    features_out[...] = jnp.concatenate(
        [features, jnp.broadcast_to(centre, (1, 128)), jnp.zeros((6, 128), F32)], axis=0
    )
    near_mean = jnp.sum(singles[...] * features, axis=1, keepdims=True) / total
    square = jnp.sum(pairs[...] * features, axis=1, keepdims=True) / total
    inv = lax.rsqrt(square - near_mean * near_mean + 1e-05)
    mean = near_mean + centre * jnp.sum(singles[...], axis=1, keepdims=True)
    lane = iota((chan, 128), 1)
    stats[0:chan] = jnp.where(lane == 0, mean, jnp.where(lane == 1, inv, 0.0))
    stats[chan : chan + 8] = jnp.broadcast_to(to_lanes(near_mean), (8, 128))
    stats[chan + 8 : chan + 16] = jnp.broadcast_to(to_lanes(inv), (8, 128))
    scale = 0.5 * to_column(params[0:1], chan) * inv
    shift = 0.5 * to_column(params[1:2], chan) - mean * scale
    stats[chan + 16 :] = jnp.where(lane == 0, scale, jnp.where(lane == 1, shift, 0.0))
    scale = jnp.broadcast_to(scale, (chan, wide))
    shift = jnp.broadcast_to(shift, (chan, wide))
    ext = w1.shape[0] // chan
    block, taps = wf.shape
    first = jnp.zeros((chan, 128), F32)
    second = jnp.zeros((chan, 128), F32)
    own_mask = usable[:, :frame_dev]
    for r in range(ext):
        value, _ = silu_halves(pre_one[r * chan : (r + 1) * chan, :] * scale + shift)
        value = value * (usable * row_valid(r - 3, rows))
        base = r * 3 * chan
        low = value.astype(BF16)
        act[base : base + chan, :] = (pltpu.roll(value, 1, 1) * behind).astype(BF16)
        act[base + chan : base + 2 * chan, :] = low
        act[base + 2 * chan : base + 3 * chan, :] = (pltpu.roll(value, wide - 1, 1) * ahead).astype(BF16)
        if 2 <= r < rows + 4:
            own_act[(r - 2) * chan : (r - 1) * chan] = low[:, :frame_dev]
        if r < 5 or (r - 5) % 4:
            continue
        g = (r - 5) // 4
        result = dot(wf[...], act[g * 3 * block : g * 3 * block + taps, :])
        pre_two[g * block : (g + 1) * block] = result
        for q in range(4):
            if 2 <= 4 * g + q < rows + 2:
                p = result[q * chan : (q + 1) * chan, :frame_dev]
                masked = p * own_mask
                first = first + halves(masked)
                second = second + halves(masked * p)
    first = jnp.sum(first, axis=1, keepdims=True)
    second = jnp.sum(second, axis=1, keepdims=True)
    payload[...] = jnp.broadcast_to(to_lanes(first) + to_lanes(second, chan), payload.shape)


def backward_scaled(recv, pre_two, recv_mel, recv_tm, pooled_own, params, masks,
                    grad, payload, pairs_hbm, stats, up, temp, pairs, sems):
    expand(recv_mel, recv_tm, pooled_own, up, temp)
    chan = params.shape[1]
    rows = MEL_ROWS
    wide = pre_two.shape[1]
    frame_dev = wide - RIM
    usable = masks[0:1]
    total = masks[3:4, 0:1]
    sums = jnp.sum(recv[...], axis=0, keepdims=True)
    mean = to_column(sums, chan) / total
    inv = lax.rsqrt(to_column(sums, chan, chan) / total - mean * mean + 1e-05)
    lane = iota((chan, 128), 1)
    stats[...] = jnp.where(lane == 0, mean, jnp.where(lane == 1, inv, 0.0))
    mean = jnp.broadcast_to(mean, (chan, wide))
    inv = jnp.broadcast_to(inv, (chan, wide))
    scale = 0.5 * to_column(params[2:3], chan)
    shift = jnp.broadcast_to(0.5 * to_column(params[3:4], chan), (chan, wide))
    scale = jnp.broadcast_to(scale, (chan, wide))

    first = jnp.zeros((chan, 128), F32)
    second = jnp.zeros((chan, 128), F32)
    own_mask = usable[:, :frame_dev]
    stores = []
    for q in list(range(2, rows + 2)) + [0, 1, rows + 2, rows + 3]:
        r = q // 2
        at = slice(q * chan, (q + 1) * chan)
        mask = usable * (0.5 * row_valid(q - 2, rows))
        normed = (pre_two[at, :] - mean) * inv
        value, slope = silu_halves(normed * scale + shift)
        g = up[r * chan : (r + 1) * chan, :] * slope * mask
        grad[at, :] = g
        if 2 <= q < rows + 2:
            g = g[:, :frame_dev]
            first = first + halves(g * normed[:, :frame_dev])
            second = second + halves(g)
            value = value[:, :frame_dev] * own_mask
            both = value if q % 2 == 0 else both + value
            if q % 2:
                pairs[(r - 1) * chan : r * chan, :] = both
                if r % 2 == 0:
                    part = pl.ds((r - 2) * chan, 2 * chan)
                    stores.append(
                        pltpu.make_async_copy(pairs.at[part, :], pairs_hbm.at[part, :], sems.at[r // 2 - 1])
                    )
                    stores[-1].start()
    first = jnp.sum(first, axis=1, keepdims=True)
    second = jnp.sum(second, axis=1, keepdims=True)
    payload[...] = jnp.broadcast_to(to_lanes(first) + to_lanes(second, chan), payload.shape)
    for store in stores:
        store.wait()


def pool(after, pairs_hbm, out, temp, pairs, sem):
    del after
    load = pltpu.make_async_copy(pairs_hbm, pairs, sem)
    load.start()
    chan, rows, half = out.shape[1:]
    to_mean = jnp.where(iota((2 * half, half), 0) >> 1 == iota((2 * half, half), 1), 0.25, 0.0)
    load.wait()
    pooled = dot(pairs[...], to_mean, precision=EXACT)
    for r in range(rows):
        temp[pl.ds(r, chan, stride=rows), :] = pooled[r * chan : (r + 1) * chan]
    out[0] = temp[...].reshape(chan, rows, half).astype(BF16)


def backward_two(recv, pre_two, grad, stats, params, masks, act, out, payload, gain_out, bias_out, shifted):
    chan = params.shape[1]
    rows = MEL_ROWS
    wide = pre_two.shape[1]
    frame_dev = wide - RIM
    usable, behind, ahead = (masks[n : n + 1] for n in range(3))
    behind, ahead = behind[:, :frame_dev], ahead[:, :frame_dev]
    total = masks[3:4, 0:1]
    sums = jnp.sum(recv[...], axis=0, keepdims=True)
    gain_out[...] = sums[:, :chan]
    bias_out[...] = sums[:, chan:]
    mean, inv = stats[:, 0:1], stats[:, 1:2]
    factor = to_column(params[2:3], chan) * inv
    gain_part = jnp.broadcast_to(to_column(sums, chan) / total * inv, (chan, wide))
    bias_part = jnp.broadcast_to(to_column(sums, chan, chan) / total, (chan, wide))
    mean = jnp.broadcast_to(mean, (chan, wide))
    factor = jnp.broadcast_to(factor, (chan, wide))
    count = pre_two.shape[0] // chan

    table = jnp.zeros((3 * chan, 3 * chan), F32)
    for q in range(count):
        at = slice(q * chan, (q + 1) * chan)
        mask = usable * row_valid(q - 2, rows)
        centred = grad[at, :] - (bias_part + (pre_two[at, :] - mean) * gain_part) * mask
        value = factor * centred
        low = value.astype(BF16)
        out[at, :] = low
        m = q - 2
        if not 0 <= m < rows:
            continue
        base = m * 3 * chan
        shifted[base : base + chan, :] = (pltpu.roll(value, 1, 1)[:, :frame_dev] * behind).astype(BF16)
        shifted[base + chan : base + 2 * chan, :] = low[:, :frame_dev]
        shifted[base + 2 * chan : base + 3 * chan, :] = (
            pltpu.roll(value, wide - 1, 1)[:, :frame_dev] * ahead
        ).astype(BF16)
        if m % 4 == 3:
            four = range(m - 3, m + 1)
            left = jnp.concatenate([shifted[n * 3 * chan : (n + 1) * 3 * chan, :] for n in four], axis=1)
            right = jnp.concatenate([act[n * chan : (n + 3) * chan, :] for n in four], axis=1)
            table = table + dot(left, right, ((1,), (1,)))
    payload[0 : 3 * chan] = table[:, :128]
    upper = 3 * chan // 2
    payload[3 * chan :] = jnp.concatenate([table[:upper, 128:], table[upper:, 128:]], axis=1)


def backward_one(grad, w1, x3, stats, params, masks, wb_hbm, out, sums, g3, pre_one, wb, g1, sem):
    fetch = pltpu.make_async_copy(wb_hbm, wb, sem)
    fetch.start()
    chan = wb.shape[0] // 4
    rows = MEL_ROWS
    wide = x3.shape[1]
    frame_dev = wide - RIM
    usable, behind, ahead = (masks[n : n + 1] for n in range(3))
    block = wb.shape[0]
    count = grad.shape[0] // chan
    pre_one[...] = dot(w1[2 * chan : (rows + 4) * chan], x3[...])

    scale = jnp.broadcast_to(stats[chan + 16 :, 0:1], (chan, wide))
    shift = jnp.broadcast_to(stats[chan + 16 :, 1:2], (chan, wide))
    factor = jnp.broadcast_to(to_column(params[0:1], chan) * stats[0:chan, 1:2], (chan, wide))
    fetch.wait()
    for q in range(count):
        low = grad[q * chan : (q + 1) * chan, :]
        value = low.astype(F32)
        base = q * 3 * chan
        g3[base : base + chan, :] = (pltpu.roll(value, 1, 1) * behind).astype(BF16)
        g3[base + chan : base + 2 * chan, :] = low
        g3[base + 2 * chan : base + 3 * chan, :] = (pltpu.roll(value, wide - 1, 1) * ahead).astype(BF16)
        if q < count - 1 and (q < 5 or (q - 5) % 4):
            continue
        start = 4 * ((q - 2) // 4)
        step = min(4, rows + 2 - start)
        result = dot(
            wb[: step * chan, : (step + 2) * 3 * chan], g3[start * 3 * chan : (start + step + 2) * 3 * chan, :]
        )
        for n in range(step):
            at = slice((start + n) * chan, (start + n + 1) * chan)
            _, slope = silu_halves(pre_one[at, :] * scale + shift)
            mask = usable * (0.5 * row_valid(start + n - 1, rows))
            value = result[n * chan : (n + 1) * chan] * slope * mask
            out[at, :] = (value * factor).astype(BF16)
            g1[at, :] = value[:, :frame_dev]
    table = jnp.zeros((chan, 128), F32)
    for g in range(rows // 4):
        part = g1[chan + g * block : chan + (g + 1) * block, :]
        high = lax.reduce_precision(part, 8, 7)
        low = (part - high).astype(BF16)
        taps_in = x3[:, :frame_dev]
        products = dot(high.astype(BF16), taps_in, ((1,), (1,))) + dot(low, taps_in, ((1,), (1,)))
        for m in range(4):
            table = table + pltpu.roll(products[m * chan : (m + 1) * chan], 128 - (4 * g + m + 3), 1)
    tap = iota((16, 128), 0)
    lane = iota((16, 128), 1)
    i = (tap * 11) >> 5
    select = ((lane == BAND * (tap - 3 * i) + i) & (tap < 9)) | ((lane == 3 * BAND) & (tap == 9))
    rows10 = dot(select.astype(F32), table, ((1,), (1,)), EXACT)
    sums[...] = jnp.concatenate(
        [jnp.concatenate([rows10[0:5], rows10[5:10]], axis=1), jnp.zeros((3, 128), F32)], axis=0
    )


def collect(recv, sums, out):
    count = out.shape[0] // 14
    share = recv.shape[0] // count
    mine = recv[0:share, :]
    for d in range(1, count):
        mine = mine + recv[share * d : share * (d + 1), :]
    block = jnp.concatenate([sums[0:5], mine] + [jnp.zeros((9 - share, 128), F32)] * (share < 9), axis=0)
    for d in range(count):
        out[14 * d : 14 * (d + 1), :] = block


def transposed(low, w1, x3, stats, masks, after, ws_hbm, first, normed, ws, pre_one, sem):
    del after
    load = pltpu.make_async_copy(ws_hbm, ws, sem)
    load.start()
    chan = low.shape[0] // (MEL_ROWS + 2)
    wide = low.shape[1]
    pre_one[...] = dot(w1[2 * chan : (MEL_ROWS + 4) * chan], x3[...])
    mean = jnp.broadcast_to(stats[0:chan, 0:1], (chan, wide))
    inv = jnp.broadcast_to(stats[0:chan, 1:2], (chan, wide))
    for q in range(MEL_ROWS + 2):
        at = slice(q * chan, (q + 1) * chan)
        mask = masks[0:1] * row_valid(q - 1, MEL_ROWS)
        normed[at, :] = ((pre_one[at, :] - mean) * inv * mask).astype(BF16)
    load.wait()
    first[...] = dot(ws[...], low[...])


def finish(recv, features, stats, k1t, first, normed, ws, params, masks,
           spec_hbm, kernel_one_hbm, kernel_two_hbm, gain_hbm, bias_hbm,
           table, spec_grad, kernel_one, kernel_two, gain_out, bias_out, sems):
    chan = params.shape[1]
    rows = MEL_ROWS
    wide = normed.shape[1]
    frame_dev = wide - RIM
    usable, behind, ahead = (masks[n : n + 1] for n in range(3))
    total = masks[3:4, 0:1]
    gain = params[0:1]
    count = recv.shape[0] // 14
    share = -(-9 * chan * chan // 128 // count)
    sums = recv[0:5, :]
    for d in range(1, count):
        sums = sums + recv[14 * d : 14 * d + 5, :]
    ten = jnp.concatenate([sums[:, :chan], sums[:, chan:]], axis=0)
    bias_sum = ten[9:10]
    mean_l, inv_l = stats[chan : chan + 1, :chan], stats[chan + 8 : chan + 9, :chan]
    ten = ten - features[1:2, 0:1] * bias_sum
    k = k1t[0:9]
    gain_sum = inv_l * (jnp.sum(k * ten[0:9], axis=0, keepdims=True) - mean_l * bias_sum)
    gain_out[...] = gain_sum
    bias_out[...] = bias_sum
    stores = [
        pltpu.make_async_copy(gain_out, gain_hbm, sems.at[0]),
        pltpu.make_async_copy(bias_out, bias_hbm, sems.at[1]),
    ]
    stores[0].start()
    stores[1].start()
    factor_l = gain * inv_l
    scale = factor_l * gain_sum / total
    scale = jnp.concatenate([scale, scale], axis=1)
    scale = jnp.concatenate([scale] * ((rows + 2) // 2), axis=1)
    taps = first[...] - dot((ws[...].astype(F32) * scale).astype(BF16), normed[...])
    for part in range(wide // 128):
        table[part] = taps[:, 128 * part : 128 * (part + 1)]
    moved = [
        jnp.concatenate([table[part, pl.ds(b, rows, stride=8), :] for part in range(wide // 128)], axis=1)
        for b in range(3)
    ]
    constant = jnp.sum(k * (factor_l * bias_sum / total), axis=1, keepdims=True)
    for a in range(3):
        row = iota((rows, 1), 0) + (a - 1) + lax.axis_index("mel") * rows
        valid = ((row >= 0) & (row < lax.axis_size("mel") * rows)).astype(F32) * usable
        for b in range(3):
            t = 3 * (2 - a) + 2 - b
            moved[b] = moved[b] - constant[t : t + 1] * valid
    result = pltpu.roll(moved[0], 1, 1) * behind + moved[1] + pltpu.roll(moved[2], wide - 1, 1) * ahead
    spec_grad[0] = (result * usable)[:, :frame_dev]
    stores.append(pltpu.make_async_copy(spec_grad, spec_hbm, sems.at[2]))
    stores[-1].start()
    whole = jnp.concatenate([recv[14 * d + 5 : 14 * d + 5 + share, :] for d in range(count)], axis=0)
    upper = 3 * chan // 2
    main = whole[: 3 * chan]
    rest = whole[3 * chan : 3 * chan + upper]
    last = jnp.concatenate([rest[:, :chan], rest[:, chan:]], axis=0)
    for j in range(3):
        at = slice((2 - j) * chan, (3 - j) * chan)
        kernel_two[j] = main[at, :chan]
        kernel_two[3 + j] = main[at, chan:]
        kernel_two[6 + j] = last[at]
    stores.append(pltpu.make_async_copy(kernel_two, kernel_two_hbm, sems.at[3]))
    stores[-1].start()
    row = features[0:1, :]
    lane = iota((1, 128), 1)
    gram = jnp.concatenate(
        [jnp.where(lane < 9, pltpu.roll(row, 128 - 9 * t, 1) if t else row, 0.0) for t in range(9)]
        + [jnp.zeros((7, 128), F32)],
        axis=0,
    )
    single = to_column(row, 16, 81)[0:9]
    k_rows = jnp.concatenate([k1t[...], jnp.zeros((112, chan), F32)], axis=0)
    normed_taps = inv_l * (dot(gram, k_rows, precision=EXACT)[0:9] - single * mean_l)
    grad_taps = factor_l * (ten[0:9] - (bias_sum * single + gain_sum * normed_taps) / total)
    for i in range(3):
        kernel_one[i] = grad_taps[3 * i : 3 * i + 3]
    stores.append(pltpu.make_async_copy(kernel_one, kernel_one_hbm, sems.at[4]))
    stores[-1].start()
    for store in stores:
        store.wait()


def run(kernel, outs, scratch, *args, hbm=0, apart=(), flops=10**8, size=4 * 10**6):
    vmem = pl.BlockSpec(memory_space=pltpu.VMEM)
    specs = []
    args = list(args)
    for n, a in enumerate(args):
        if hbm and n >= len(args) - hbm:
            specs.append(pl.BlockSpec(memory_space=pltpu.HBM))
            args[n] = pltpu.with_memory_space_constraint(a, pltpu.HBM)
        else:
            specs.append(vmem)
            args[n] = pltpu.with_memory_space_constraint(a, pltpu.VMEM)
    return pl.pallas_call(
        kernel,
        out_shape=outs,
        in_specs=specs,
        out_specs=[pl.BlockSpec(memory_space=pltpu.HBM) if n in apart else vmem for n in range(len(outs))],
        scratch_shapes=scratch,
        compiler_params=pltpu.CompilerParams(vmem_limit_bytes=30 * 2**20),
        cost_estimate=pl.CostEstimate(flops=flops, bytes_accessed=size, transcendentals=0),
    )(*args)


def shape(dims, dtype=F32):
    return jax.ShapeDtypeStruct(dims, dtype)


def kept(dims, dtype=F32):
    return pltpu.VMEM(dims, dtype)


def far(dims, dtype=F32):
    return pltpu.HBM(dims, dtype)


def exchange(blocks, axes=AXES):
    return lax.all_to_all(blocks, axes, 0, 0, tiled=True)


def exchange_rows(rows, axes=AXES):
    return exchange(rows[:, None, :], axes)[:, 0, :]


def shards(spectrum, clip_bounds, kernel_one, gain_one, bias_one, kernel_two, gain_two, bias_two, pooled_grad):
    _, rows, frame_dev = spectrum.shape
    chan = kernel_two.shape[0]
    n_mel, n_tm = lax.axis_size("mel"), lax.axis_size("tm")
    devices = n_mel * n_tm
    half = frame_dev // 2
    wide = frame_dev + RIM
    mels = n_mel * rows

    packed, own = run(
        pack_mel,
        [kept((n_mel, 2 * rows + chan, half), BF16), kept(pooled_grad.shape, BF16)],
        [
            pltpu.VMEM(spectrum.shape, BF16),
            pltpu.SemaphoreType.DMA((2,)),
        ],
        spectrum,
        pooled_grad,
        hbm=2,
    )
    recv_mel = exchange(packed, "mel")
    ext = rows + 6
    span = 6 * 3 * chan
    wf, wb, w1, ws, pairs, singles, k1t, params, masks, edge_masks, twice = run(
        weights,
        [
            kept((4 * chan, span), BF16),
            far((4 * chan, span), BF16),
            kept((ext * chan, 128), BF16),
            far((rows * 8, (rows + 2) * chan), BF16),
            kept((chan, 128)),
            kept((chan, 128)),
            kept((16, chan)),
            kept((8, chan)),
            kept((8, wide)),
            kept((n_tm * 8, 128)),
            kept((128, 128)),
        ],
        [
            pltpu.VMEM((9, chan, chan), BF16),
            pltpu.VMEM((3, 3, chan), BF16),
            pltpu.VMEM((4, 1, chan), F32),
            pltpu.SMEM(clip_bounds.shape, jnp.int32),
            pltpu.VMEM((4 * chan, span), BF16),
            pltpu.VMEM((rows * 8, (rows + 2) * chan), BF16),
            pltpu.SemaphoreType.DMA((9,)),
        ],
        clip_bounds,
        jnp.transpose(kernel_two, (2, 3, 0, 1)).reshape(9, chan, chan),
        jnp.transpose(kernel_one, (1, 2, 0)),
        gain_one[None],
        bias_one[None],
        gain_two[None],
        bias_two[None],
        hbm=7,
        apart=(1, 3),
    )
    (packed,) = run(
        pack_tm,
        [kept((n_tm, 16, 128), BF16)],
        [pltpu.VMEM((n_tm * 16, 128), F32)],
        recv_mel,
        own,
        masks,
    )
    recv_tm = exchange(packed, "tm")
    pre_two, payload, act, x3, stats_one, features = run(
        forward_one,
        [
            kept(((rows + 4) * chan, wide)),
            kept((devices, 128)),
            kept(((rows + 2) * chan, frame_dev), BF16),
            kept((128, wide), BF16),
            kept((2 * chan + 16, 128)),
            kept((8, 128)),
        ],
        [
            pltpu.VMEM((ext * 3 * chan, wide), BF16),
            pltpu.VMEM((ext * chan, wide), F32),
            pltpu.VMEM((mels + 8, wide), F32),
        ],
        recv_mel,
        recv_tm,
        pairs,
        singles,
        twice,
        w1,
        wf,
        params,
        masks,
        edge_masks,
    )
    recv = exchange_rows(payload)
    grad, payload, row_pairs, stats_two = run(
        backward_scaled,
        [
            kept(((rows + 4) * chan, wide)),
            kept((devices, 128)),
            far((rows // 2 * chan, frame_dev)),
            kept((chan, 128)),
        ],
        [
            pltpu.VMEM(((rows // 2 + 2) * chan, wide), F32),
            pltpu.VMEM((rows // 2 * chan, 128), F32),
            pltpu.VMEM((rows // 2 * chan, frame_dev), F32),
            pltpu.SemaphoreType.DMA((rows // 4,)),
        ],
        recv,
        pre_two,
        recv_mel,
        recv_tm,
        own,
        params,
        masks,
        apart=(2,),
    )
    recv = exchange_rows(payload)
    pieces = 9 * chan * chan // 128
    grad, payload, gain_two_grad, bias_two_grad = run(
        backward_two,
        [kept(((rows + 4) * chan, wide), BF16), kept((pieces, 128)), shape((1, chan)), shape((1, chan))],
        [pltpu.VMEM((rows * 3 * chan, frame_dev), BF16)],
        recv,
        pre_two,
        grad,
        stats_two,
        params,
        masks,
        act,
    )
    share = -(-pieces // devices)
    if share * devices > pieces:
        payload = jnp.pad(payload, ((0, share * devices - pieces), (0, 0)))
    recv = exchange_rows(payload)
    low, sums = run(
        backward_one,
        [kept(((rows + 2) * chan, wide), BF16), kept((8, 128))],
        [
            pltpu.VMEM(((rows + 4) * 3 * chan, wide), BF16),
            pltpu.VMEM(((rows + 2) * chan, wide), F32),
            pltpu.VMEM((4 * chan, span), BF16),
            pltpu.VMEM(((rows + 2) * chan, frame_dev), F32),
            pltpu.SemaphoreType.DMA,
        ],
        grad,
        w1,
        x3,
        stats_one,
        params,
        masks,
        wb,
        hbm=1,
    )
    (payload,) = run(collect, [kept((devices * 14, 128))], [], recv, sums)
    recv = exchange_rows(payload)
    (pooled,) = run(
        pool,
        [shape((1, chan, rows // 2, half), BF16)],
        [
            pltpu.VMEM((rows // 2 * chan, 128), F32),
            pltpu.VMEM((rows // 2 * chan, frame_dev), F32),
            pltpu.SemaphoreType.DMA,
        ],
        sums,
        row_pairs,
        hbm=1,
    )
    first, normed, ws = run(
        transposed,
        [
            kept((rows * 8, wide)),
            kept(((rows + 2) * chan, wide), BF16),
            kept((rows * 8, (rows + 2) * chan), BF16),
        ],
        [pltpu.VMEM(((rows + 2) * chan, wide), F32), pltpu.SemaphoreType.DMA],
        low,
        w1,
        x3,
        stats_one,
        masks,
        sums,
        ws,
        hbm=1,
    )
    spec_grad, kernel_one_grad, kernel_two_grad, gain_one_grad, bias_one_grad = run(
        finish,
        [
            shape((1, rows, frame_dev)),
            shape((3, 3, chan)),
            shape((9, chan, chan)),
            shape((1, chan)),
            shape((1, chan)),
        ],
        [
            pltpu.VMEM((3, rows * 8, 128), F32),
            pltpu.VMEM((1, rows, frame_dev), F32),
            pltpu.VMEM((3, 3, chan), F32),
            pltpu.VMEM((9, chan, chan), F32),
            pltpu.VMEM((1, chan), F32),
            pltpu.VMEM((1, chan), F32),
            pltpu.SemaphoreType.DMA((5,)),
        ],
        recv,
        features,
        stats_one,
        k1t,
        first,
        normed,
        ws,
        params,
        masks,
        apart=range(5),
    )
    kernel_two_grad = jnp.transpose(kernel_two_grad.reshape(3, 3, chan, chan), (2, 3, 0, 1))
    return (
        pooled,
        spec_grad,
        jnp.transpose(kernel_one_grad, (2, 0, 1)),
        gain_one_grad[0],
        bias_one_grad[0],
        kernel_two_grad,
        gain_two_grad[0],
        bias_two_grad[0],
    )


def solution(mesh):
    return jax.shard_map(
        shards,
        mesh=mesh,
        in_specs=(
            P(None, "mel", "tm"),
            P(),
            P(),
            P(),
            P(),
            P(),
            P(),
            P(),
            P(None, None, "mel", "tm"),
        ),
        out_specs=(P(None, None, "mel", "tm"), P(None, "mel", "tm"), P(), P(), P(), P(), P(), P()),
        check_vma=False,
    )
```

```python
import functools

import jax
import jax.numpy as jnp
from jax import lax
from jax.experimental import pallas as pl
from jax.experimental.pallas import tpu as pltpu
from jax.sharding import PartitionSpec as P

F32 = jnp.float32
BF16 = jnp.bfloat16
AXES = ("mel", "tm")
EXACT = lax.Precision.HIGHEST
RIM = 128
BAND = 24
MEL_ROWS = 16


def iota(shape, dim):
    return lax.broadcasted_iota(jnp.int32, shape, dim)


def dot(a, b, over=((1,), (0,)), precision=None):
    return lax.dot_general(a, b, (over, ((), ())), precision=precision, preferred_element_type=F32)


def to_column(lanes, count, start=0):
    shape = (count, lanes.shape[1])
    return jnp.sum(jnp.where(iota(shape, 1) == iota(shape, 0) + start, lanes, 0.0), axis=1, keepdims=True)


def to_lanes(column, start=0, width=128):
    shape = (column.shape[0], width)
    return jnp.sum(jnp.where(iota(shape, 1) == iota(shape, 0) + start, column, 0.0), axis=0, keepdims=True)


def halves(v):
    return sum(v[:, n : n + 128] for n in range(128, v.shape[1], 128)) + v[:, :128]


def frame_masks(bounds, frames):
    last = bounds.shape[1] - 1

    def living(f):
        return (f >= 0) & (f < bounds[0, last])

    def paired(f):
        both = living(f) & living(f + 1)
        for k in range(1, last):
            both = both & (f + 1 != bounds[0, k])
        return both

    return tuple(m.astype(F32) for m in (living(frames), paired(frames - 1), paired(frames)))


def row_valid(row, rows):
    mel = lax.axis_index("mel") * rows + row
    return ((mel >= 0) & (mel < lax.axis_size("mel") * rows)).astype(F32)


def load_all(*pairs, sems):
    copies = [pltpu.make_async_copy(src, dst, sems.at[n]) for n, (src, dst) in enumerate(pairs)]
    for copy in copies:
        copy.start()
    for copy in copies:
        copy.wait()


def pack_mel(spec_hbm, grad_hbm, out, own, spec, sems):
    load_all((spec_hbm, spec), (grad_hbm, own), sems=sems)
    me = lax.axis_index("mel")
    x = spec[0]
    rows, frame_dev = x.shape
    half = frame_dev // 2
    g = own[0].astype(F32)
    top = g[:, 0, :]
    bottom = g[:, g.shape[1] - 1, :]
    for j in range(out.shape[0]):
        out[j, 0:rows] = x[:, :half]
        out[j, rows : 2 * rows] = x[:, half:]
        edge = jnp.where(j == me - 1, top, 0.0) + jnp.where(j == me + 1, bottom, 0.0)
        out[j, 2 * rows :] = edge.astype(BF16)


def weights(bounds_hbm, k2_hbm, k1_hbm, gain_one_hbm, bias_one_hbm, gain_two_hbm, bias_two_hbm,
            wf, wb_hbm, w1, ws_hbm, pairs, singles, k1t, params, masks, edge_masks, twice,
            k2, k1, vectors, bounds, wb, ws, sems):
    load_all(
        (bounds_hbm, bounds),
        (k2_hbm, k2),
        (k1_hbm, k1),
        (gain_one_hbm, vectors.at[0]),
        (bias_one_hbm, vectors.at[1]),
        (gain_two_hbm, vectors.at[2]),
        (bias_two_hbm, vectors.at[3]),
        sems=sems,
    )
    chan = k2.shape[1]
    span = wf.shape[1]
    wide = masks.shape[1]
    frame_dev = wide - RIM
    lane = iota((1, wide), 1)
    frames = lax.axis_index("tm") * frame_dev + jnp.where(lane < frame_dev + RIM // 2, lane, lane - wide)
    last = bounds.shape[1] - 1
    pixels = (bounds[0, last] * (lax.axis_size("mel") * MEL_ROWS)).astype(F32)
    masks[...] = jnp.concatenate(
        list(frame_masks(bounds, frames)) + [jnp.full((1, wide), 1.0) * pixels, jnp.zeros((4, wide), F32)], axis=0
    )
    q = iota(edge_masks.shape, 0)
    lane = iota(edge_masks.shape, 1)
    k = q % 8
    frames = (q // 8) * frame_dev + jnp.where(k < 4, k, k + frame_dev - 8)
    living, behind, ahead = frame_masks(bounds, frames)
    living = jnp.where((k == 0) | (k == 7), living, 0.0)
    edge_masks[...] = jnp.where(lane == 0, living, jnp.where(lane == 1, behind, jnp.where(lane == 2, ahead, 0.0)))
    params[...] = jnp.concatenate(
        [vectors[n] for n in range(4)] + [jnp.zeros((4, chan), F32)], axis=0
    )
    tap = iota((16, 128), 0)
    lane = iota((16, 128), 1)
    i = (tap * 11) >> 5
    ninth = (lane * 57) >> 9
    to_band = (lane == BAND * (tap - 3 * i) + i) & (tap < 9)
    to_left = (ninth == tap) & (tap < 9)
    to_right = (lane - 9 * ninth == tap) & (lane < 81)
    to_single = (lane == 81 + tap) & (tap < 9)
    source = iota((128, 128), 0) - 81
    lane = iota((128, 128), 1)
    ninth = (lane * 57) >> 9
    inside = (source >= 0) & (source < 9) & (lane < 81)
    twice[...] = jnp.where(inside, (source == ninth).astype(F32) + (source == lane - 9 * ninth).astype(F32), 0.0)
    taps = [k2[t].astype(F32) for t in range(9)]
    rest = jnp.zeros((chan, span - 9 * chan), F32)
    forward = jnp.concatenate(taps + [rest], axis=1)
    backward = jnp.concatenate([taps[8 - t].T for t in range(9)] + [rest], axis=1)
    for r in range(wb.shape[0] // chan):
        at = slice(r * chan, (r + 1) * chan)
        wb[at] = (pltpu.roll(backward, 3 * chan * r, 1) if r else backward).astype(BF16)
    store_wb = pltpu.make_async_copy(wb, wb_hbm, sems.at[7])
    store_wb.start()
    for r in range(wf.shape[0] // chan):
        at = slice(r * chan, (r + 1) * chan)
        wf[at] = (pltpu.roll(forward, 3 * chan * r, 1) if r else forward).astype(BF16)
    full = jnp.concatenate([k1[n].astype(F32) for n in range(3)] + [jnp.zeros((7, chan), F32)], axis=0)
    k1t[...] = full
    k = full.astype(BF16)
    lanes = [dot(k, select.astype(BF16), ((0,), (0,))) for select in (to_band, to_left, to_right, to_single)]
    pairs[...] = lanes[1] * lanes[2]
    singles[...] = lanes[3]
    for m in range(w1.shape[0] // chan):
        w1[m * chan : (m + 1) * chan] = (pltpu.roll(lanes[0], m, 1) if m else lanes[0]).astype(BF16)
    low = [
        jnp.concatenate([full[3 * (2 - a) + 2 - b : 3 * (2 - a) + 3 - b] for a in range(3)], axis=1)
        for b in range(3)
    ]
    base = jnp.concatenate(low + [jnp.zeros((5, 3 * chan), F32)], axis=0)
    base = jnp.concatenate([base, jnp.zeros((8, ws.shape[1] - 3 * chan), F32)], axis=1)
    for m in range(ws.shape[0] // 8):
        ws[8 * m : 8 * m + 8] = (pltpu.roll(base, chan * m, 1) if m else base).astype(BF16)
    store_ws = pltpu.make_async_copy(ws, ws_hbm, sems.at[8])
    store_ws.start()
    store_wb.wait()
    store_ws.wait()


def feature_rows(shifted, axis_shift, weight, centre):
    z = [None] * 9
    for j in range(3):
        for i in range(3):
            z[3 * i + j] = axis_shift(shifted[j], i) - centre

    def folded(v):
        if v.shape[1] > 128:
            v = v[:, :128] + v[:, 128:]
        return jnp.sum(v, axis=0, keepdims=True)

    rows = [None] * 96
    for s in range(9):
        left = z[s] * weight
        rows[81 + s] = folded(left)
        for t in range(s, 9):
            rows[9 * s + t] = rows[9 * t + s] = folded(left * z[t])
    zero = jnp.zeros((1, 128), F32)
    stack = jnp.concatenate([zero if r is None else r for r in rows], axis=0)
    return to_lanes(jnp.sum(stack, axis=1, keepdims=True))


def flat_rows(own):
    _, chan, rows, half = own.shape
    return own[0].astype(F32).reshape(chan * rows, half).astype(BF16)


def pack_tm(recv, own, masks, out, spread):
    count = out.shape[0]
    n_mel = recv.shape[0]
    me_m, me_t = lax.axis_index("mel"), lax.axis_index("tm")
    rows = MEL_ROWS
    half = recv.shape[2]
    frame_dev = 2 * half
    mels = n_mel * rows
    lane = iota((1, frame_dev), 1)
    usable, behind, ahead = (masks[n : n + 1, :frame_dev] for n in range(3))
    x = jnp.concatenate(
        [
            jnp.concatenate([recv[j, 0:rows] for j in range(n_mel)], axis=0),
            jnp.concatenate([recv[j, rows : 2 * rows] for j in range(n_mel)], axis=0),
        ],
        axis=1,
    )
    x = x.astype(F32) * usable
    inner = jnp.where((lane > 0) & (lane < frame_dev - 1), usable, 0.0)
    number = mels * jnp.sum(inner, axis=1, keepdims=True)
    centre = jnp.sum(jnp.sum(x, axis=0, keepdims=True), axis=1, keepdims=True)
    centre = centre / (mels * jnp.maximum(jnp.sum(usable, axis=1, keepdims=True), 1.0))
    centre = lax.reduce_precision(centre, 8, 7)
    row = iota((mels, frame_dev), 0)

    def mel_shift(v, i):
        if i == 1:
            return v
        if i == 0:
            return jnp.where(row == 0, 0.0, pltpu.roll(v, 1, 0))
        return jnp.where(row == mels - 1, 0.0, pltpu.roll(v, mels - 1, 0))

    shifted = [pltpu.roll(x, 1, 1) * behind, x, pltpu.roll(x, frame_dev - 1, 1) * ahead]
    features = feature_rows(shifted, mel_shift, inner, centre)
    lane = iota((1, 128), 1)
    features = jnp.where(lane == 90, centre, jnp.where(lane == 91, number, features))
    high = lax.reduce_precision(features, 8, 7)
    mid = lax.reduce_precision(features - high, 8, 7)
    low = features - high - mid
    pick = iota((8, frame_dev), 0)
    column = jnp.where(pick < 4, pick, frame_dev - 8 + pick)
    edges = dot((iota((8, frame_dev), 1) == column).astype(BF16), x.astype(BF16), ((1,), (1,)))
    edges = jnp.concatenate([edges, jnp.zeros((8, 128 - mels), F32)], axis=1)
    target = iota((count, half), 0)
    at = iota((count, half), 1)
    choose = ((target == me_t - 1) & (at == 0)) | ((target == me_t + 1) & (at == half - 1))
    choose = choose.astype(BF16)
    above = recv[jnp.maximum(me_m - 1, 0), 2 * rows :]
    below = recv[jnp.minimum(me_m + 1, n_mel - 1), 2 * rows :]
    columns = dot(choose, flat_rows(own), ((1,), (1,)))
    outer = jnp.concatenate([dot(choose, above, ((1,), (1,))), dot(choose, below, ((1,), (1,)))], axis=1)
    parts = columns.shape[1] // 128
    for q in range(parts):
        spread[pl.ds(8 + q, count, stride=16), :] = columns[:, 128 * q : 128 * (q + 1)]
    spread[pl.ds(8 + parts, count, stride=16), :] = outer
    common = jnp.concatenate([high, mid, low], axis=0)
    for j in range(count):
        tail = jnp.concatenate([spread[16 * j + 8 : 16 * j + 13, :], common], axis=0)
        out[j] = jnp.concatenate([edges, tail], axis=0).astype(BF16)


def expand(recv_mel, recv_tm, own, out, temp):
    me_m, me_t = lax.axis_index("mel"), lax.axis_index("tm")
    n_mel, count = recv_mel.shape[0], recv_tm.shape[0]
    chan, rows, half = own.shape[1:]
    wide = out.shape[1]
    above = recv_mel[jnp.maximum(me_m - 1, 0), 2 * MEL_ROWS :]
    below = recv_mel[jnp.minimum(me_m + 1, n_mel - 1), 2 * MEL_ROWS :]
    every = jnp.concatenate([flat_rows(own), above, below], axis=0)
    after = recv_tm[jnp.minimum(me_t + 1, count - 1)].astype(F32)
    before = recv_tm[jnp.maximum(me_t - 1, 0)].astype(F32)
    after = jnp.concatenate([after[8 + q : 9 + q] for q in range(5)], axis=1)
    before = jnp.concatenate([before[8 + q : 9 + q] for q in range(5)], axis=1)
    side = iota((16, after.shape[1]), 0)
    sides = jnp.where(side == 0, after, jnp.where(side == 1, before, 0.0)).astype(BF16)
    lane = iota((half, wide), 1)
    spread = jnp.where((lane >> 1 == iota((half, wide), 0)) & (lane < 2 * half), 0.25, 0.0).astype(BF16)
    lane = iota((16, wide), 1)
    side = iota((16, wide), 0)
    right = (side == 0) & (lane >= 2 * half) & (lane < 2 * half + 2)
    left = (side == 1) & (lane >= wide - 2)
    columns = jnp.where(right | left, 0.25, 0.0).astype(BF16)
    full = dot(every, spread) + dot(sides, columns, ((0,), (0,)))
    for part in range(wide // 128):
        cut = slice(128 * part, 128 * (part + 1))
        temp[...] = full[: chan * rows, cut]
        for r in range(rows):
            out[(r + 1) * chan : (r + 2) * chan, cut] = temp[pl.ds(r, chan, stride=rows), :]
    out[0:chan] = full[chan * rows : chan * (rows + 1)]
    out[(rows + 1) * chan :] = full[chan * (rows + 1) :]


def silu_halves(h):
    t = jnp.tanh(h)
    one = 1.0 + t
    return h * one, one * (1.0 + h * (1.0 - t))


def forward_one(recv_mel, recv_tm, pairs, singles, twice, w1, wf, params, masks, edge_masks,
                pre_two, payload, act, x3, stats, features_out, pre_one, xs):
    n_mel, count = recv_mel.shape[0], recv_tm.shape[0]
    rows = MEL_ROWS
    mels = n_mel * rows
    half = recv_mel.shape[2]
    frame_dev = 2 * half
    wide = frame_dev + RIM
    chan = params.shape[1]
    me_m, me_t = lax.axis_index("mel"), lax.axis_index("tm")
    usable, behind, ahead = (masks[n : n + 1] for n in range(3))
    total = masks[3:4, 0:1]
    x = jnp.concatenate(
        [
            jnp.concatenate([recv_mel[j, 0:rows] for j in range(n_mel)], axis=0),
            jnp.concatenate([recv_mel[j, rows : 2 * rows] for j in range(n_mel)], axis=0),
        ],
        axis=1,
    ).astype(F32)
    after = recv_tm[jnp.minimum(me_t + 1, count - 1)].astype(F32)[0:8, :mels]
    before = recv_tm[jnp.maximum(me_t - 1, 0)].astype(F32)[0:8, :mels]
    after = jnp.where(me_t + 1 < count, after, 0.0)
    before = jnp.where(me_t > 0, before, 0.0)
    sides = jnp.concatenate([after[0:4], before[4:8], jnp.zeros((8, mels), F32)], axis=0).astype(BF16)
    side = iota((16, RIM), 0)
    place = iota((16, RIM), 1) == jnp.where(side < 4, side, jnp.where(side < 8, side + RIM - 8, -1))
    x = jnp.concatenate([x, dot(sides, place.astype(BF16), ((0,), (0,)))], axis=1) * usable
    xs[0:8] = jnp.zeros((8, wide), F32)
    xs[mels : mels + 8] = jnp.zeros((8, wide), F32)
    xs[4 : mels + 4] = x
    near = xs[pl.ds(pl.multiple_of(me_m * rows, 8), BAND), :]
    x3[...] = jnp.concatenate(
        [
            pltpu.roll(near, 1, 1) * behind,
            near,
            pltpu.roll(near, wide - 1, 1) * ahead,
            jnp.broadcast_to(usable, (BAND, wide)),
            jnp.zeros((128 - 4 * BAND, wide), F32),
        ],
        axis=0,
    ).astype(BF16)
    pre_one[...] = dot(w1[...], x3[...])
    parts = [recv_tm[d].astype(F32)[8:16] for d in range(count)]
    parts = [p[5:6] + p[6:7] + p[7:8] for p in parts]
    centres = [p[:, 90:91] for p in parts]
    numbers = [p[:, 91:92] for p in parts]
    weight = functools.reduce(jnp.add, numbers)
    centre = functools.reduce(jnp.add, [c * n for c, n in zip(centres, numbers)]) / jnp.maximum(weight, 1.0)
    lane = iota((1, 128), 1)
    features = jnp.zeros((1, 128), F32)
    moved = jnp.zeros((1, 128), F32)
    for part, c, n in zip(parts, centres, numbers):
        delta = c - centre
        moved = moved + delta * part
        features = features + part + delta * n * jnp.where(lane < 81, delta, 1.0)
    moved = dot(jnp.broadcast_to(moved, (8, 128)), twice[...], precision=EXACT)[0:1]
    features = features + moved
    edge = recv_tm[:, 0:8, :].astype(F32).reshape(count * 8, 128)
    q_usable, q_behind, q_ahead = (edge_masks[:, n : n + 1] for n in range(3))
    lane = iota((count * 8, 128), 1)

    def lane_shift(v, i):
        if i == 1:
            return v
        if i == 0:
            return jnp.where(lane < mels, pltpu.roll(v, 1, 1), 0.0)
        return pltpu.roll(v, 127, 1)

    shifted = [
        pltpu.roll(edge, 1, 0) * q_behind,
        edge,
        pltpu.roll(edge, count * 8 - 1, 0) * q_ahead,
    ]
    features = features + feature_rows(shifted, lane_shift, jnp.where(lane < mels, q_usable, 0.0), centre)
    features = jnp.where(iota((1, 128), 1) < 90, features, 0.0)
    features_out[...] = jnp.concatenate(
        [features, jnp.broadcast_to(centre, (1, 128)), jnp.zeros((6, 128), F32)], axis=0
    )
    near_mean = jnp.sum(singles[...] * features, axis=1, keepdims=True) / total
    square = jnp.sum(pairs[...] * features, axis=1, keepdims=True) / total
    inv = lax.rsqrt(square - near_mean * near_mean + 1e-05)
    mean = near_mean + centre * jnp.sum(singles[...], axis=1, keepdims=True)
    lane = iota((chan, 128), 1)
    stats[0:chan] = jnp.where(lane == 0, mean, jnp.where(lane == 1, inv, 0.0))
    stats[chan : chan + 8] = jnp.broadcast_to(to_lanes(near_mean), (8, 128))
    stats[chan + 8 : chan + 16] = jnp.broadcast_to(to_lanes(inv), (8, 128))
    scale = 0.5 * to_column(params[0:1], chan) * inv
    shift = 0.5 * to_column(params[1:2], chan) - mean * scale
    stats[chan + 16 :] = jnp.where(lane == 0, scale, jnp.where(lane == 1, shift, 0.0))
    scale = jnp.broadcast_to(scale, (chan, wide))
    shift = jnp.broadcast_to(shift, (chan, wide))
    ext = w1.shape[0] // chan
    block, taps = wf.shape
    first = jnp.zeros((chan, 128), F32)
    second = jnp.zeros((chan, 128), F32)
    own_mask = usable[:, :frame_dev]
    for r in range(ext):
        value, _ = silu_halves(pre_one[r * chan : (r + 1) * chan, :] * scale + shift)
        value = value * (usable * row_valid(r - 3, rows))
        base = r * 3 * chan
        low = value.astype(BF16)
        act[base : base + chan, :] = (pltpu.roll(value, 1, 1) * behind).astype(BF16)
        act[base + chan : base + 2 * chan, :] = low
        act[base + 2 * chan : base + 3 * chan, :] = (pltpu.roll(value, wide - 1, 1) * ahead).astype(BF16)
        if r < 5 or (r - 5) % 4:
            continue
        g = (r - 5) // 4
        result = dot(wf[...], act[g * 3 * block : g * 3 * block + taps, :])
        pre_two[g * block : (g + 1) * block] = result
        for q in range(4):
            if 2 <= 4 * g + q < rows + 2:
                p = result[q * chan : (q + 1) * chan, :frame_dev]
                masked = p * own_mask
                first = first + halves(masked)
                second = second + halves(masked * p)
    first = jnp.sum(first, axis=1, keepdims=True)
    second = jnp.sum(second, axis=1, keepdims=True)
    payload[...] = jnp.broadcast_to(to_lanes(first) + to_lanes(second, chan), payload.shape)


def sum_rows(devices, taps):
    return -(-taps // devices) + 2


def backward_scaled(recv, pre_two, act, recv_mel, recv_tm, pooled_own, params, masks,
                    grad, payload, pairs_hbm, stats, up, temp, pairs, right, sems):
    expand(recv_mel, recv_tm, pooled_own, up, temp)
    chan = params.shape[1]
    rows = MEL_ROWS
    wide = pre_two.shape[1]
    frame_dev = wide - RIM
    usable = masks[0:1]
    total = masks[3:4, 0:1]
    sums = jnp.sum(recv[...], axis=0, keepdims=True)
    mean = to_column(sums, chan) / total
    inv = lax.rsqrt(to_column(sums, chan, chan) / total - mean * mean + 1e-05)
    lane = iota((chan, 128), 1)
    stats[0:chan] = jnp.where(lane == 0, mean, jnp.where(lane == 1, inv, 0.0))
    stats[chan : chan + 8] = jnp.broadcast_to(to_lanes(inv), (8, 128))
    mean = jnp.broadcast_to(mean, (chan, wide))
    inv = jnp.broadcast_to(inv, (chan, wide))
    scale = 0.5 * to_column(params[2:3], chan)
    shift = jnp.broadcast_to(0.5 * to_column(params[3:4], chan), (chan, wide))
    scale = jnp.broadcast_to(scale, (chan, wide))
    first = jnp.zeros((chan, 128), F32)
    second = jnp.zeros((chan, 128), F32)
    own_mask = usable[:, :frame_dev]
    right[3 * chan :] = jnp.ones((16, rows * frame_dev), BF16)
    table = jnp.zeros((9 * chan, 3 * chan + 16), F32)
    stores = []
    for q in list(range(2, rows + 2)) + [0, 1, rows + 2, rows + 3]:
        r = q // 2
        at = slice(q * chan, (q + 1) * chan)
        mask = usable * (0.5 * row_valid(q - 2, rows))
        normed = (pre_two[at, :] - mean) * inv
        value, slope = silu_halves(normed * scale + shift)
        g = up[r * chan : (r + 1) * chan, :] * slope * mask
        grad[at, :] = g
        m = q - 2
        if not 0 <= m < rows:
            continue
        g = g[:, :frame_dev]
        normed = normed[:, :frame_dev]
        first = first + halves(g * normed)
        second = second + halves(g)
        value = value[:, :frame_dev] * own_mask
        both = value if q % 2 == 0 else both + value
        if q % 2:
            pairs[(r - 1) * chan : r * chan, :] = both
            if r % 2 == 0:
                part = pl.ds((r - 2) * chan, 2 * chan)
                stores.append(pltpu.make_async_copy(pairs.at[part, :], pairs_hbm.at[part, :], sems.at[r // 2 - 1]))
                stores[-1].start()
        lanes = slice(m * frame_dev, (m + 1) * frame_dev)
        high = lax.reduce_precision(g, 8, 7)
        right[0:chan, lanes] = high.astype(BF16)
        right[chan : 2 * chan, lanes] = (g - high).astype(BF16)
        right[2 * chan : 3 * chan, lanes] = normed.astype(BF16)
        if m % 4 == 3:
            left = [act[(n + 2) * 3 * chan : (n + 5) * 3 * chan, :frame_dev] for n in range(m - 3, m + 1)]
            lanes = slice((m - 3) * frame_dev, (m + 1) * frame_dev)
            table = table + dot(jnp.concatenate(left, axis=1), right[:, lanes], ((1,), (1,)))
    first = jnp.sum(first, axis=1, keepdims=True)
    second = jnp.sum(second, axis=1, keepdims=True)
    totals = to_lanes(first) + to_lanes(second, chan)
    devices = recv.shape[0]
    block = payload.shape[0] // devices
    payload[pl.ds(0, devices, stride=block), :] = jnp.broadcast_to(totals, (devices, 128))
    both = jnp.concatenate([table[:, :chan] + table[:, chan : 2 * chan], table[:, 2 * chan : 3 * chan]], axis=1)
    single = table[:, 3 * chan : 3 * chan + 1]
    lane = iota((devices, 128), 1)
    constants = jnp.zeros((devices, 128), F32)
    for k in range(block - 2):
        cut, ones = both[k * devices : (k + 1) * devices], single[k * devices : (k + 1) * devices]
        short = devices - cut.shape[0]
        if short:
            cut = jnp.concatenate([cut, jnp.zeros((short, 128), F32)], axis=0)
            ones = jnp.concatenate([ones, jnp.zeros((short, 1), F32)], axis=0)
        payload[pl.ds(1 + k, devices, stride=block), :] = cut
        constants = jnp.where(lane == k, ones, constants)
    payload[pl.ds(block - 1, devices, stride=block), :] = constants
    for store in stores:
        store.wait()


def pool(after, pairs_hbm, out, temp, pairs, sem):
    del after
    load = pltpu.make_async_copy(pairs_hbm, pairs, sem)
    load.start()
    chan, rows, half = out.shape[1:]
    to_mean = jnp.where(iota((2 * half, half), 0) >> 1 == iota((2 * half, half), 1), 0.25, 0.0)
    load.wait()
    pooled = dot(pairs[...], to_mean, precision=EXACT)
    for r in range(rows):
        temp[pl.ds(r, chan, stride=rows), :] = pooled[r * chan : (r + 1) * chan]
    out[0] = temp[...].reshape(chan, rows, half).astype(BF16)


def backward(recv, pre_two, grad, stats_two, w1, x3, stats, params, masks, wb_hbm,
             out, payload, gain_out, bias_out, g3, pre_one, g1, wb, sem):
    fetch = pltpu.make_async_copy(wb_hbm, wb, sem)
    fetch.start()
    chan = params.shape[1]
    rows = MEL_ROWS
    wide = pre_two.shape[1]
    frame_dev = wide - RIM
    usable, behind, ahead = (masks[n : n + 1] for n in range(3))
    total = masks[3:4, 0:1]
    devices = payload.shape[0] // 14
    block = recv.shape[0] // devices
    pre_one[...] = dot(w1[2 * chan : (rows + 4) * chan], x3[...])

    def summed(k):
        return jnp.sum(recv[pl.ds(k, devices, stride=block), :], axis=0, keepdims=True)

    sums = summed(0)
    gain_sum, bias_sum = sums[:, :chan], sums[:, chan:]
    gain_out[...] = gain_sum
    bias_out[...] = bias_sum
    share = block - 2
    mine = jnp.concatenate([summed(1 + k) for k in range(share)], axis=0)
    single = to_column(summed(block - 1), share)
    factor_l = params[2:3] * stats_two[chan : chan + 1, :chan]
    mine = mine[:, :chan] - (bias_sum * single + gain_sum * mine[:, chan:]) / total
    mine = factor_l * mine
    lower = -(-share // 2)
    mine = jnp.concatenate([mine] + [jnp.zeros((2 * lower - share, chan), F32)] * (share % 2), axis=0)
    mine = jnp.concatenate([mine[:lower], mine[lower:]], axis=1)
    if lower < 9:
        mine = jnp.concatenate([mine, jnp.zeros((9 - lower, 128), F32)], axis=0)
    mean, inv = stats_two[0:chan, 0:1], stats_two[0:chan, 1:2]
    factor = to_column(params[2:3], chan) * inv
    gain_part = jnp.broadcast_to(to_column(sums, chan) / total * inv, (chan, wide))
    bias_part = jnp.broadcast_to(to_column(sums, chan, chan) / total, (chan, wide))
    mean = jnp.broadcast_to(mean, (chan, wide))
    factor = jnp.broadcast_to(factor, (chan, wide))
    scale = jnp.broadcast_to(stats[chan + 16 :, 0:1], (chan, wide))
    shift = jnp.broadcast_to(stats[chan + 16 :, 1:2], (chan, wide))
    factor_one = jnp.broadcast_to(to_column(params[0:1], chan) * stats[0:chan, 1:2], (chan, wide))
    count = pre_two.shape[0] // chan
    table = jnp.zeros((chan, 128), F32)
    for q in range(count):
        at = slice(q * chan, (q + 1) * chan)
        mask = usable * row_valid(q - 2, rows)
        centred = grad[at, :] - (bias_part + (pre_two[at, :] - mean) * gain_part) * mask
        value = factor * centred
        base = q * 3 * chan
        g3[base : base + chan, :] = (pltpu.roll(value, 1, 1) * behind).astype(BF16)
        g3[base + chan : base + 2 * chan, :] = value.astype(BF16)
        g3[base + 2 * chan : base + 3 * chan, :] = (pltpu.roll(value, wide - 1, 1) * ahead).astype(BF16)
        if q == 5:
            fetch.wait()
        if q < count - 1 and (q < 5 or (q - 5) % 4):
            continue
        start = 4 * ((q - 2) // 4)
        step = min(4, rows + 2 - start)
        result = dot(
            wb[: step * chan, : (step + 2) * 3 * chan], g3[start * 3 * chan : (start + step + 2) * 3 * chan, :]
        )
        for n in range(step):
            m = start + n - 1
            at = slice((m + 1) * chan, (m + 2) * chan)
            _, slope = silu_halves(pre_one[at, :] * scale + shift)
            mask = usable * (0.5 * row_valid(m, rows))
            value = result[n * chan : (n + 1) * chan] * slope * mask
            out[at, :] = (value * factor_one).astype(BF16)
            if not 0 <= m < rows:
                continue
            g1[m * chan : (m + 1) * chan, :] = value[:, :frame_dev]
            if m % 4 == 3:
                part = g1[(m - 3) * chan : (m + 1) * chan, :]
                high = lax.reduce_precision(part, 8, 7)
                low = (part - high).astype(BF16)
                taps_in = x3[:, :frame_dev]
                products = dot(high.astype(BF16), taps_in, ((1,), (1,))) + dot(low, taps_in, ((1,), (1,)))
                for k in range(4):
                    table = table + pltpu.roll(products[k * chan : (k + 1) * chan], 128 - (m + k), 1)
    tap = iota((16, 128), 0)
    lane = iota((16, 128), 1)
    i = (tap * 11) >> 5
    select = ((lane == BAND * (tap - 3 * i) + i) & (tap < 9)) | ((lane == 3 * BAND) & (tap == 9))
    rows10 = dot(select.astype(F32), table, ((1,), (1,)), EXACT)
    sums = jnp.concatenate([rows10[0:5], rows10[5:10]], axis=1)
    block = jnp.concatenate([sums, mine], axis=0)
    for d in range(devices):
        payload[14 * d : 14 * (d + 1), :] = block


def transposed(low, w1, x3, stats, masks, ws_hbm, first, normed, ws, pre_one, sem):
    load = pltpu.make_async_copy(ws_hbm, ws, sem)
    load.start()
    chan = low.shape[0] // (MEL_ROWS + 2)
    wide = low.shape[1]
    pre_one[...] = dot(w1[2 * chan : (MEL_ROWS + 4) * chan], x3[...])
    mean = jnp.broadcast_to(stats[0:chan, 0:1], (chan, wide))
    inv = jnp.broadcast_to(stats[0:chan, 1:2], (chan, wide))
    for q in range(MEL_ROWS + 2):
        at = slice(q * chan, (q + 1) * chan)
        mask = masks[0:1] * row_valid(q - 1, MEL_ROWS)
        normed[at, :] = ((pre_one[at, :] - mean) * inv * mask).astype(BF16)
    load.wait()
    first[...] = dot(ws[...], low[...])


def finish(recv, features, stats, k1t, first, normed, ws, params, masks,
           spec_hbm, kernel_one_hbm, kernel_two_hbm, gain_hbm, bias_hbm,
           table, spec_grad, kernel_one, kernel_two, gain_out, bias_out, sems):
    chan = params.shape[1]
    rows = MEL_ROWS
    wide = normed.shape[1]
    frame_dev = wide - RIM
    usable, behind, ahead = (masks[n : n + 1] for n in range(3))
    total = masks[3:4, 0:1]
    gain = params[0:1]
    count = recv.shape[0] // 14
    share = -(-9 * chan // count)
    sums = recv[0:5, :]
    for d in range(1, count):
        sums = sums + recv[14 * d : 14 * d + 5, :]
    ten = jnp.concatenate([sums[:, :chan], sums[:, chan:]], axis=0)
    bias_sum = ten[9:10]
    mean_l, inv_l = stats[chan : chan + 1, :chan], stats[chan + 8 : chan + 9, :chan]
    ten = ten - features[1:2, 0:1] * bias_sum
    k = k1t[0:9]
    gain_sum = inv_l * (jnp.sum(k * ten[0:9], axis=0, keepdims=True) - mean_l * bias_sum)
    gain_out[...] = gain_sum
    bias_out[...] = bias_sum
    stores = [
        pltpu.make_async_copy(gain_out, gain_hbm, sems.at[0]),
        pltpu.make_async_copy(bias_out, bias_hbm, sems.at[1]),
    ]
    stores[0].start()
    stores[1].start()
    factor_l = gain * inv_l
    scale = factor_l * gain_sum / total
    scale = jnp.concatenate([scale, scale], axis=1)
    scale = jnp.concatenate([scale] * ((rows + 2) // 2), axis=1)
    taps = first[...] - dot((ws[...].astype(F32) * scale).astype(BF16), normed[...])
    for part in range(wide // 128):
        table[part] = taps[:, 128 * part : 128 * (part + 1)]
    moved = [
        jnp.concatenate([table[part, pl.ds(b, rows, stride=8), :] for part in range(wide // 128)], axis=1)
        for b in range(3)
    ]
    constant = jnp.sum(k * (factor_l * bias_sum / total), axis=1, keepdims=True)
    for a in range(3):
        row = iota((rows, 1), 0) + (a - 1) + lax.axis_index("mel") * rows
        valid = ((row >= 0) & (row < lax.axis_size("mel") * rows)).astype(F32) * usable
        for b in range(3):
            t = 3 * (2 - a) + 2 - b
            moved[b] = moved[b] - constant[t : t + 1] * valid
    result = pltpu.roll(moved[0], 1, 1) * behind + moved[1] + pltpu.roll(moved[2], wide - 1, 1) * ahead
    spec_grad[0] = (result * usable)[:, :frame_dev]
    stores.append(pltpu.make_async_copy(spec_grad, spec_hbm, sems.at[2]))
    stores[-1].start()
    lower = -(-share // 2)
    left = [recv[pl.ds(5 + p, count, stride=14), :] for p in range(lower)]
    whole = jnp.concatenate([v[:, :chan] for v in left] + [v[:, chan:] for v in left], axis=0)
    for t in range(9):
        kernel_two[t] = whole[t * chan : (t + 1) * chan].T
    stores.append(pltpu.make_async_copy(kernel_two, kernel_two_hbm, sems.at[3]))
    stores[-1].start()
    row = features[0:1, :]
    lane = iota((1, 128), 1)
    gram = jnp.concatenate(
        [jnp.where(lane < 9, pltpu.roll(row, 128 - 9 * t, 1) if t else row, 0.0) for t in range(9)]
        + [jnp.zeros((7, 128), F32)],
        axis=0,
    )
    single = to_column(row, 16, 81)[0:9]
    k_rows = jnp.concatenate([k1t[...], jnp.zeros((112, chan), F32)], axis=0)
    normed_taps = inv_l * (dot(gram, k_rows, precision=EXACT)[0:9] - single * mean_l)
    grad_taps = factor_l * (ten[0:9] - (bias_sum * single + gain_sum * normed_taps) / total)
    for i in range(3):
        kernel_one[i] = grad_taps[3 * i : 3 * i + 3]
    stores.append(pltpu.make_async_copy(kernel_one, kernel_one_hbm, sems.at[4]))
    stores[-1].start()
    for store in stores:
        store.wait()


def run(kernel, outs, scratch, *args, hbm=0, apart=(), flops=10**8, size=4 * 10**6):
    vmem = pl.BlockSpec(memory_space=pltpu.VMEM)
    specs = []
    args = list(args)
    for n, a in enumerate(args):
        if hbm and n >= len(args) - hbm:
            specs.append(pl.BlockSpec(memory_space=pltpu.HBM))
            args[n] = pltpu.with_memory_space_constraint(a, pltpu.HBM)
        else:
            specs.append(vmem)
            args[n] = pltpu.with_memory_space_constraint(a, pltpu.VMEM)
    return pl.pallas_call(
        kernel,
        out_shape=outs,
        in_specs=specs,
        out_specs=[pl.BlockSpec(memory_space=pltpu.HBM) if n in apart else vmem for n in range(len(outs))],
        scratch_shapes=scratch,
        compiler_params=pltpu.CompilerParams(vmem_limit_bytes=30 * 2**20),
        cost_estimate=pl.CostEstimate(flops=flops, bytes_accessed=size, transcendentals=0),
    )(*args)


def shape(dims, dtype=F32):
    return jax.ShapeDtypeStruct(dims, dtype)


def kept(dims, dtype=F32):
    return pltpu.VMEM(dims, dtype)


def far(dims, dtype=F32):
    return pltpu.HBM(dims, dtype)


def exchange(blocks, axes=AXES):
    return lax.all_to_all(blocks, axes, 0, 0, tiled=True)


def exchange_rows(rows, axes=AXES):
    return exchange(rows[:, None, :], axes)[:, 0, :]


def shards(spectrum, clip_bounds, kernel_one, gain_one, bias_one, kernel_two, gain_two, bias_two, pooled_grad):
    _, rows, frame_dev = spectrum.shape
    chan = kernel_two.shape[0]
    n_mel, n_tm = lax.axis_size("mel"), lax.axis_size("tm")
    devices = n_mel * n_tm
    half = frame_dev // 2
    wide = frame_dev + RIM
    mels = n_mel * rows

    packed, own = run(
        pack_mel,
        [kept((n_mel, 2 * rows + chan, half), BF16), kept(pooled_grad.shape, BF16)],
        [
            pltpu.VMEM(spectrum.shape, BF16),
            pltpu.SemaphoreType.DMA((2,)),
        ],
        spectrum,
        pooled_grad,
        hbm=2,
    )
    recv_mel = exchange(packed, "mel")
    ext = rows + 6
    span = 6 * 3 * chan
    wf, wb, w1, ws, pairs, singles, k1t, params, masks, edge_masks, twice = run(
        weights,
        [
            kept((4 * chan, span), BF16),
            far((4 * chan, span), BF16),
            kept((ext * chan, 128), BF16),
            far((rows * 8, (rows + 2) * chan), BF16),
            kept((chan, 128)),
            kept((chan, 128)),
            kept((16, chan)),
            kept((8, chan)),
            kept((8, wide)),
            kept((n_tm * 8, 128)),
            kept((128, 128)),
        ],
        [
            pltpu.VMEM((9, chan, chan), BF16),
            pltpu.VMEM((3, 3, chan), BF16),
            pltpu.VMEM((4, 1, chan), F32),
            pltpu.SMEM(clip_bounds.shape, jnp.int32),
            pltpu.VMEM((4 * chan, span), BF16),
            pltpu.VMEM((rows * 8, (rows + 2) * chan), BF16),
            pltpu.SemaphoreType.DMA((9,)),
        ],
        clip_bounds,
        jnp.transpose(kernel_two, (2, 3, 0, 1)).reshape(9, chan, chan),
        jnp.transpose(kernel_one, (1, 2, 0)),
        gain_one[None],
        bias_one[None],
        gain_two[None],
        bias_two[None],
        hbm=7,
        apart=(1, 3),
    )
    (packed,) = run(
        pack_tm,
        [kept((n_tm, 16, 128), BF16)],
        [pltpu.VMEM((n_tm * 16, 128), F32)],
        recv_mel,
        own,
        masks,
    )
    recv_tm = exchange(packed, "tm")
    pre_two, payload, act, x3, stats_one, features = run(
        forward_one,
        [
            kept(((rows + 4) * chan, wide)),
            kept((devices, 128)),
            kept((ext * 3 * chan, wide), BF16),
            kept((128, wide), BF16),
            kept((2 * chan + 16, 128)),
            kept((8, 128)),
        ],
        [pltpu.VMEM((ext * chan, wide), F32), pltpu.VMEM((mels + 8, wide), F32)],
        recv_mel,
        recv_tm,
        pairs,
        singles,
        twice,
        w1,
        wf,
        params,
        masks,
        edge_masks,
    )
    recv = exchange_rows(payload)
    grad, payload, row_pairs, stats_two = run(
        backward_scaled,
        [
            kept(((rows + 4) * chan, wide)),
            kept((devices * sum_rows(devices, 9 * chan), 128)),
            far((rows // 2 * chan, frame_dev)),
            kept((chan + 8, 128)),
        ],
        [
            pltpu.VMEM(((rows // 2 + 2) * chan, wide), F32),
            pltpu.VMEM((rows // 2 * chan, 128), F32),
            pltpu.VMEM((rows // 2 * chan, frame_dev), F32),
            pltpu.VMEM((3 * chan + 16, rows * frame_dev), BF16),
            pltpu.SemaphoreType.DMA((rows // 4,)),
        ],
        recv,
        pre_two,
        act,
        recv_mel,
        recv_tm,
        own,
        params,
        masks,
        apart=(2,),
    )
    recv = exchange_rows(payload)
    low, payload, gain_two_grad, bias_two_grad = run(
        backward,
        [
            kept(((rows + 2) * chan, wide), BF16),
            kept((devices * 14, 128)),
            shape((1, chan)),
            shape((1, chan)),
        ],
        [
            pltpu.VMEM(((rows + 4) * 3 * chan, wide), BF16),
            pltpu.VMEM(((rows + 2) * chan, wide), F32),
            pltpu.VMEM((rows * chan, frame_dev), F32),
            pltpu.VMEM((4 * chan, span), BF16),
            pltpu.SemaphoreType.DMA,
        ],
        recv,
        pre_two,
        grad,
        stats_two,
        w1,
        x3,
        stats_one,
        params,
        masks,
        wb,
        hbm=1,
    )
    recv = exchange_rows(payload)
    (pooled,) = run(
        pool,
        [shape((1, chan, rows // 2, half), BF16)],
        [
            pltpu.VMEM((rows // 2 * chan, 128), F32),
            pltpu.VMEM((rows // 2 * chan, frame_dev), F32),
            pltpu.SemaphoreType.DMA,
        ],
        payload,
        row_pairs,
        hbm=1,
    )
    first, normed, ws = run(
        transposed,
        [
            kept((rows * 8, wide)),
            kept(((rows + 2) * chan, wide), BF16),
            kept((rows * 8, (rows + 2) * chan), BF16),
        ],
        [pltpu.VMEM(((rows + 2) * chan, wide), F32), pltpu.SemaphoreType.DMA],
        low,
        w1,
        x3,
        stats_one,
        masks,
        ws,
        hbm=1,
    )
    spec_grad, kernel_one_grad, kernel_two_grad, gain_one_grad, bias_one_grad = run(
        finish,
        [
            shape((1, rows, frame_dev)),
            shape((3, 3, chan)),
            shape((9, chan, chan)),
            shape((1, chan)),
            shape((1, chan)),
        ],
        [
            pltpu.VMEM((3, rows * 8, 128), F32),
            pltpu.VMEM((1, rows, frame_dev), F32),
            pltpu.VMEM((3, 3, chan), F32),
            pltpu.VMEM((9, chan, chan), F32),
            pltpu.VMEM((1, chan), F32),
            pltpu.VMEM((1, chan), F32),
            pltpu.SemaphoreType.DMA((5,)),
        ],
        recv,
        features,
        stats_one,
        k1t,
        first,
        normed,
        ws,
        params,
        masks,
        apart=range(5),
    )
    kernel_two_grad = jnp.transpose(kernel_two_grad.reshape(3, 3, chan, chan), (2, 3, 0, 1))
    return (
        pooled,
        spec_grad,
        jnp.transpose(kernel_one_grad, (2, 0, 1)),
        gain_one_grad[0],
        bias_one_grad[0],
        kernel_two_grad,
        gain_two_grad[0],
        bias_two_grad[0],
    )


def solution(mesh):
    return jax.shard_map(
        shards,
        mesh=mesh,
        in_specs=(
            P(None, "mel", "tm"),
            P(),
            P(),
            P(),
            P(),
            P(),
            P(),
            P(),
            P(None, None, "mel", "tm"),
        ),
        out_specs=(P(None, None, "mel", "tm"), P(None, "mel", "tm"), P(), P(), P(), P(), P(), P()),
        check_vma=False,
    )
```

```python
import functools

import jax
import jax.numpy as jnp
from jax import lax
from jax.experimental import pallas as pl
from jax.experimental.pallas import tpu as pltpu
from jax.sharding import PartitionSpec as P

F32 = jnp.float32
BF16 = jnp.bfloat16
AXES = ("mel", "tm")
EXACT = lax.Precision.HIGHEST
RIM = 128
BAND = 24
MEL_ROWS = 16


def iota(shape, dim):
    return lax.broadcasted_iota(jnp.int32, shape, dim)


def dot(a, b, over=((1,), (0,)), precision=None):
    return lax.dot_general(a, b, (over, ((), ())), precision=precision, preferred_element_type=F32)


def to_column(lanes, count, start=0):
    shape = (count, lanes.shape[1])
    return jnp.sum(jnp.where(iota(shape, 1) == iota(shape, 0) + start, lanes, 0.0), axis=1, keepdims=True)


def to_lanes(column, start=0, width=128):
    shape = (column.shape[0], width)
    return jnp.sum(jnp.where(iota(shape, 1) == iota(shape, 0) + start, column, 0.0), axis=0, keepdims=True)


def halves(v):
    return sum(v[:, n : n + 128] for n in range(128, v.shape[1], 128)) + v[:, :128]


def frame_masks(bounds, frames):
    last = bounds.shape[1] - 1

    def living(f):
        return (f >= 0) & (f < bounds[0, last])

    def paired(f):
        both = living(f) & living(f + 1)
        for k in range(1, last):
            both = both & (f + 1 != bounds[0, k])
        return both

    return tuple(m.astype(F32) for m in (living(frames), paired(frames - 1), paired(frames)))


def row_valid(row, rows):
    mel = lax.axis_index("mel") * rows + row
    return ((mel >= 0) & (mel < lax.axis_size("mel") * rows)).astype(F32)


def start_all(*pairs, sems):
    copies = [pltpu.make_async_copy(src, dst, sems.at[n]) for n, (src, dst) in enumerate(pairs)]
    for copy in copies:
        copy.start()
    return copies


def wait_all(copies):
    for copy in copies:
        copy.wait()


def shifted_frames(value, behind, ahead):
    wide = value.shape[1]
    return pltpu.roll(value, 1, 1) * behind, pltpu.roll(value, wide - 1, 1) * ahead


def pack_mel(spec_hbm, grad_hbm, out, own, spec, sems):
    wait_all(start_all((spec_hbm, spec), (grad_hbm, own), sems=sems))
    me = lax.axis_index("mel")
    x = spec[0]
    rows, frame_dev = x.shape
    half = frame_dev // 2
    g = own[0].astype(F32)
    top = g[:, 0, :]
    bottom = g[:, g.shape[1] - 1, :]
    for j in range(out.shape[0]):
        out[j, 0:rows] = x[:, :half]
        out[j, rows : 2 * rows] = x[:, half:]
        edge = jnp.where(j == me - 1, top, 0.0) + jnp.where(j == me + 1, bottom, 0.0)
        out[j, 2 * rows :] = edge.astype(BF16)


def weights(own, bounds_hbm, k2_hbm, k1_hbm, gain_one_hbm, bias_one_hbm, gain_two_hbm, bias_two_hbm,
            wf, wb_hbm, w1, ws_hbm, pairs, singles, k1t, params, masks, edge_masks, twice, own_rows,
            k2, k1, vectors, bounds, wb, ws, temp, sems):
    loads = start_all(
        (bounds_hbm, bounds),
        (k2_hbm, k2),
        (k1_hbm, k1),
        (gain_one_hbm, vectors.at[0]),
        (bias_one_hbm, vectors.at[1]),
        (gain_two_hbm, vectors.at[2]),
        (bias_two_hbm, vectors.at[3]),
        sems=sems,
    )
    _, many, count, half = own.shape
    temp[...] = own[0].astype(F32).reshape(many * count, half)
    for r in range(count):
        own_rows[r * many : (r + 1) * many] = temp[pl.ds(r, many, stride=count), :].astype(BF16)
    wait_all(loads)
    chan = k2.shape[1]
    span = wf.shape[1]
    taps = [k2[t].astype(F32) for t in range(9)]
    rest = jnp.zeros((chan, span - 9 * chan), F32)
    forward = jnp.concatenate(taps + [rest], axis=1)
    backward = jnp.concatenate([taps[8 - t].T for t in range(9)] + [rest], axis=1)
    for r in range(wb.shape[0] // chan):
        at = slice(r * chan, (r + 1) * chan)
        wb[at] = (pltpu.roll(backward, 3 * chan * r, 1) if r else backward).astype(BF16)
    store_wb = pltpu.make_async_copy(wb, wb_hbm, sems.at[7])
    store_wb.start()
    full = jnp.concatenate([k1[n].astype(F32) for n in range(3)] + [jnp.zeros((7, chan), F32)], axis=0)
    low = [
        jnp.concatenate([full[3 * (2 - a) + 2 - b : 3 * (2 - a) + 3 - b] for a in range(3)], axis=1)
        for b in range(3)
    ]
    base = jnp.concatenate(low + [jnp.zeros((5, 3 * chan), F32)], axis=0)
    base = jnp.concatenate([base, jnp.zeros((8, ws.shape[1] - 3 * chan), F32)], axis=1)
    for m in range(ws.shape[0] // 8):
        ws[8 * m : 8 * m + 8] = (pltpu.roll(base, chan * m, 1) if m else base).astype(BF16)
    store_ws = pltpu.make_async_copy(ws, ws_hbm, sems.at[8])
    store_ws.start()
    wide = masks.shape[1]
    frame_dev = wide - RIM
    lane = iota((1, wide), 1)
    frames = lax.axis_index("tm") * frame_dev + jnp.where(lane < frame_dev + RIM // 2, lane, lane - wide)
    last = bounds.shape[1] - 1
    pixels = (bounds[0, last] * (lax.axis_size("mel") * MEL_ROWS)).astype(F32)
    masks[...] = jnp.concatenate(
        list(frame_masks(bounds, frames)) + [jnp.full((1, wide), 1.0) * pixels, jnp.zeros((4, wide), F32)], axis=0
    )
    q = iota(edge_masks.shape, 0)
    lane = iota(edge_masks.shape, 1)
    k = q % 8
    frames = (q // 8) * frame_dev + jnp.where(k < 4, k, k + frame_dev - 8)
    living, behind, ahead = frame_masks(bounds, frames)
    living = jnp.where((k == 0) | (k == 7), living, 0.0)
    edge_masks[...] = jnp.where(lane == 0, living, jnp.where(lane == 1, behind, jnp.where(lane == 2, ahead, 0.0)))
    params[...] = jnp.concatenate(
        [vectors[n] for n in range(4)] + [jnp.zeros((4, chan), F32)], axis=0
    )
    tap = iota((16, 128), 0)
    lane = iota((16, 128), 1)
    i = (tap * 11) >> 5
    ninth = (lane * 57) >> 9
    to_band = (lane == BAND * (tap - 3 * i) + i) & (tap < 9)
    to_left = (ninth == tap) & (tap < 9)
    to_right = (lane - 9 * ninth == tap) & (lane < 81)
    to_single = (lane == 81 + tap) & (tap < 9)
    source = iota((128, 128), 0) - 81
    lane = iota((128, 128), 1)
    ninth = (lane * 57) >> 9
    inside = (source >= 0) & (source < 9) & (lane < 81)
    twice[...] = jnp.where(inside, (source == ninth).astype(F32) + (source == lane - 9 * ninth).astype(F32), 0.0)
    for r in range(wf.shape[0] // chan):
        at = slice(r * chan, (r + 1) * chan)
        wf[at] = (pltpu.roll(forward, 3 * chan * r, 1) if r else forward).astype(BF16)
    k1t[...] = full
    k = full.astype(BF16)
    lanes = [dot(k, select.astype(BF16), ((0,), (0,))) for select in (to_band, to_left, to_right, to_single)]
    pairs[...] = lanes[1] * lanes[2]
    singles[...] = lanes[3]
    for m in range(w1.shape[0] // chan):
        w1[m * chan : (m + 1) * chan] = (pltpu.roll(lanes[0], m, 1) if m else lanes[0]).astype(BF16)
    store_wb.wait()
    store_ws.wait()


def feature_rows(shifted, axis_shift, weight, centre):
    z = [None] * 9
    for j in range(3):
        for i in range(3):
            z[3 * i + j] = axis_shift(shifted[j], i) - centre

    def folded(v):
        if v.shape[1] > 128:
            v = v[:, :128] + v[:, 128:]
        return jnp.sum(v, axis=0, keepdims=True)

    rows = [None] * 96
    for s in range(9):
        left = z[s] * weight
        rows[81 + s] = folded(left)
        for t in range(s, 9):
            rows[9 * s + t] = rows[9 * t + s] = folded(left * z[t])
    zero = jnp.zeros((1, 128), F32)
    stack = jnp.concatenate([zero if r is None else r for r in rows], axis=0)
    return to_lanes(jnp.sum(stack, axis=1, keepdims=True))


def pack_tm(recv, own_rows, masks, out, spread):
    count = out.shape[0]
    n_mel = recv.shape[0]
    me_m, me_t = lax.axis_index("mel"), lax.axis_index("tm")
    rows = MEL_ROWS
    half = recv.shape[2]
    frame_dev = 2 * half
    mels = n_mel * rows
    lane = iota((1, frame_dev), 1)
    usable, behind, ahead = (masks[n : n + 1, :frame_dev] for n in range(3))
    x = jnp.concatenate(
        [
            jnp.concatenate([recv[j, 0:rows] for j in range(n_mel)], axis=0),
            jnp.concatenate([recv[j, rows : 2 * rows] for j in range(n_mel)], axis=0),
        ],
        axis=1,
    )
    x = x.astype(F32) * usable
    inner = jnp.where((lane > 0) & (lane < frame_dev - 1), usable, 0.0)
    number = mels * jnp.sum(inner, axis=1, keepdims=True)
    centre = jnp.sum(jnp.sum(x, axis=0, keepdims=True), axis=1, keepdims=True)
    centre = centre / (mels * jnp.maximum(jnp.sum(usable, axis=1, keepdims=True), 1.0))
    centre = lax.reduce_precision(centre, 8, 7)
    row = iota((mels, frame_dev), 0)

    def mel_shift(v, i):
        if i == 1:
            return v
        if i == 0:
            return jnp.where(row == 0, 0.0, pltpu.roll(v, 1, 0))
        return jnp.where(row == mels - 1, 0.0, pltpu.roll(v, mels - 1, 0))

    shifted = [pltpu.roll(x, 1, 1) * behind, x, pltpu.roll(x, frame_dev - 1, 1) * ahead]
    features = feature_rows(shifted, mel_shift, inner, centre)
    lane = iota((1, 128), 1)
    features = jnp.where(lane == 90, centre, jnp.where(lane == 91, number, features))
    high = lax.reduce_precision(features, 8, 7)
    mid = lax.reduce_precision(features - high, 8, 7)
    low = features - high - mid
    pick = iota((8, frame_dev), 0)
    column = jnp.where(pick < 4, pick, frame_dev - 8 + pick)
    edges = dot((iota((8, frame_dev), 1) == column).astype(BF16), x.astype(BF16), ((1,), (1,)))
    edges = jnp.concatenate([edges, jnp.zeros((8, 128 - mels), F32)], axis=1)
    target = iota((count, half), 0)
    at = iota((count, half), 1)
    choose = ((target == me_t - 1) & (at == 0)) | ((target == me_t + 1) & (at == half - 1))
    choose = choose.astype(BF16)
    above = recv[jnp.maximum(me_m - 1, 0), 2 * rows :]
    below = recv[jnp.minimum(me_m + 1, n_mel - 1), 2 * rows :]
    columns = dot(choose, own_rows[...], ((1,), (1,)))
    outer = jnp.concatenate([dot(choose, above, ((1,), (1,))), dot(choose, below, ((1,), (1,)))], axis=1)
    parts = columns.shape[1] // 128
    for q in range(parts):
        spread[pl.ds(8 + q, count, stride=16), :] = columns[:, 128 * q : 128 * (q + 1)]
    spread[pl.ds(8 + parts, count, stride=16), :] = outer
    common = jnp.concatenate([high, mid, low], axis=0)
    for j in range(count):
        tail = jnp.concatenate([spread[16 * j + 8 : 16 * j + 13, :], common], axis=0)
        out[j] = jnp.concatenate([edges, tail], axis=0).astype(BF16)


def side_columns(recv_tm, out):
    me_t = lax.axis_index("tm")
    count = recv_tm.shape[0]
    after = recv_tm[jnp.minimum(me_t + 1, count - 1)].astype(F32)
    before = recv_tm[jnp.maximum(me_t - 1, 0)].astype(F32)
    after = jnp.concatenate([after[8 + q : 9 + q] for q in range(5)], axis=1)
    before = jnp.concatenate([before[8 + q : 9 + q] for q in range(5)], axis=1)
    side = iota((16, after.shape[1]), 0)
    sides = jnp.where(side == 0, after, jnp.where(side == 1, before, 0.0)).astype(BF16)
    lane = iota((16, RIM), 1)
    side = iota((16, RIM), 0)
    columns = ((side == 0) & (lane < 2)) | ((side == 1) & (lane >= RIM - 2))
    out[...] = dot(sides, jnp.where(columns, 0.25, 0.0).astype(BF16), ((0,), (0,)))


def silu_halves(h):
    t = jnp.tanh(h)
    one = 1.0 + t
    return h * one, one * (1.0 + h * (1.0 - t))


def forward_one(recv_mel, recv_tm, pairs, singles, twice, w1, wf, params, masks, edge_masks,
                pre_two, payload, act, x3, stats, features_out, pre_one, xs):
    n_mel, count = recv_mel.shape[0], recv_tm.shape[0]
    rows = MEL_ROWS
    mels = n_mel * rows
    half = recv_mel.shape[2]
    frame_dev = 2 * half
    wide = frame_dev + RIM
    chan = params.shape[1]
    me_m, me_t = lax.axis_index("mel"), lax.axis_index("tm")
    usable, behind, ahead = (masks[n : n + 1] for n in range(3))
    total = masks[3:4, 0:1]
    x = jnp.concatenate(
        [
            jnp.concatenate([recv_mel[j, 0:rows] for j in range(n_mel)], axis=0),
            jnp.concatenate([recv_mel[j, rows : 2 * rows] for j in range(n_mel)], axis=0),
        ],
        axis=1,
    ).astype(F32)
    after = recv_tm[jnp.minimum(me_t + 1, count - 1)].astype(F32)[0:8, :mels]
    before = recv_tm[jnp.maximum(me_t - 1, 0)].astype(F32)[0:8, :mels]
    after = jnp.where(me_t + 1 < count, after, 0.0)
    before = jnp.where(me_t > 0, before, 0.0)
    sides = jnp.concatenate([after[0:4], before[4:8], jnp.zeros((8, mels), F32)], axis=0).astype(BF16)
    side = iota((16, RIM), 0)
    place = iota((16, RIM), 1) == jnp.where(side < 4, side, jnp.where(side < 8, side + RIM - 8, -1))
    x = jnp.concatenate([x, dot(sides, place.astype(BF16), ((0,), (0,)))], axis=1) * usable
    xs[0:8] = jnp.zeros((8, wide), F32)
    xs[mels : mels + 8] = jnp.zeros((8, wide), F32)
    xs[4 : mels + 4] = x
    near = xs[pl.ds(pl.multiple_of(me_m * rows, 8), BAND), :]
    x3[...] = jnp.concatenate(
        [
            pltpu.roll(near, 1, 1) * behind,
            near,
            pltpu.roll(near, wide - 1, 1) * ahead,
            jnp.broadcast_to(usable, (BAND, wide)),
            jnp.zeros((128 - 4 * BAND, wide), F32),
        ],
        axis=0,
    ).astype(BF16)
    pre_one[...] = dot(w1[...], x3[...])
    parts = [recv_tm[d].astype(F32)[8:16] for d in range(count)]
    parts = [p[5:6] + p[6:7] + p[7:8] for p in parts]
    centres = [p[:, 90:91] for p in parts]
    numbers = [p[:, 91:92] for p in parts]
    weight = functools.reduce(jnp.add, numbers)
    centre = functools.reduce(jnp.add, [c * n for c, n in zip(centres, numbers)]) / jnp.maximum(weight, 1.0)
    lane = iota((1, 128), 1)
    features = jnp.zeros((1, 128), F32)
    moved = jnp.zeros((1, 128), F32)
    for part, c, n in zip(parts, centres, numbers):
        delta = c - centre
        moved = moved + delta * part
        features = features + part + delta * n * jnp.where(lane < 81, delta, 1.0)
    moved = dot(jnp.broadcast_to(moved, (8, 128)), twice[...], precision=EXACT)[0:1]
    features = features + moved
    edge = recv_tm[:, 0:8, :].astype(F32).reshape(count * 8, 128)
    q_usable, q_behind, q_ahead = (edge_masks[:, n : n + 1] for n in range(3))
    lane = iota((count * 8, 128), 1)

    def lane_shift(v, i):
        if i == 1:
            return v
        if i == 0:
            return jnp.where(lane < mels, pltpu.roll(v, 1, 1), 0.0)
        return pltpu.roll(v, 127, 1)

    shifted = [
        pltpu.roll(edge, 1, 0) * q_behind,
        edge,
        pltpu.roll(edge, count * 8 - 1, 0) * q_ahead,
    ]
    features = features + feature_rows(shifted, lane_shift, jnp.where(lane < mels, q_usable, 0.0), centre)
    features = jnp.where(iota((1, 128), 1) < 90, features, 0.0)
    features_out[...] = jnp.concatenate(
        [features, jnp.broadcast_to(centre, (1, 128)), jnp.zeros((6, 128), F32)], axis=0
    )
    near_mean = jnp.sum(singles[...] * features, axis=1, keepdims=True) / total
    square = jnp.sum(pairs[...] * features, axis=1, keepdims=True) / total
    inv = lax.rsqrt(square - near_mean * near_mean + 1e-05)
    mean = near_mean + centre * jnp.sum(singles[...], axis=1, keepdims=True)
    lane = iota((chan, 128), 1)
    stats[0:chan] = jnp.where(lane == 0, mean, jnp.where(lane == 1, inv, 0.0))
    stats[chan : chan + 8] = jnp.broadcast_to(to_lanes(near_mean), (8, 128))
    stats[chan + 8 : chan + 16] = jnp.broadcast_to(to_lanes(inv), (8, 128))
    scale = 0.5 * to_column(params[0:1], chan) * inv
    shift = 0.5 * to_column(params[1:2], chan) - mean * scale
    stats[chan + 16 :] = jnp.where(lane == 0, scale, jnp.where(lane == 1, shift, 0.0))
    scale = jnp.broadcast_to(scale, (chan, wide))
    shift = jnp.broadcast_to(shift, (chan, wide))
    ext = w1.shape[0] // chan
    block, taps = wf.shape
    first = jnp.zeros((chan, 128), F32)
    second = jnp.zeros((chan, 128), F32)
    own_mask = usable[:, :frame_dev]
    low_masks = [m.astype(BF16) for m in (usable, behind, ahead)]
    for r in range(ext):
        value, _ = silu_halves(pre_one[r * chan : (r + 1) * chan, :] * scale + shift)
        if not 0 <= r - 3 < rows:
            value = value * row_valid(r - 3, rows)
        base = r * 3 * chan
        low = value.astype(BF16) * low_masks[0]
        act[base : base + chan, :], act[base + 2 * chan : base + 3 * chan, :] = shifted_frames(low, *low_masks[1:])
        act[base + chan : base + 2 * chan, :] = low
        if r < 5 or (r - 5) % 4:
            continue
        g = (r - 5) // 4
        result = dot(wf[...], act[g * 3 * block : g * 3 * block + taps, :])
        pre_two[g * block : (g + 1) * block] = result
        for q in range(4):
            if 2 <= 4 * g + q < rows + 2:
                p = result[q * chan : (q + 1) * chan, :frame_dev]
                masked = p * own_mask
                first = first + halves(masked)
                second = second + halves(masked * p)
    first = jnp.sum(first, axis=1, keepdims=True)
    second = jnp.sum(second, axis=1, keepdims=True)
    payload[...] = jnp.broadcast_to(to_lanes(first) + to_lanes(second, chan), payload.shape)


def sum_rows(devices, taps):
    return -(-taps // devices) + 2


def backward_scaled(recv, pre_two, act, recv_mel, recv_tm, own_rows, params, masks,
                    grad, payload, pairs_hbm, stats, sides, pairs, right, sems):
    side_columns(recv_tm, sides)
    me_m, n_mel = lax.axis_index("mel"), recv_mel.shape[0]
    chan = params.shape[1]
    half = own_rows.shape[1]
    lane = iota((half, 2 * half), 1)
    spread = jnp.where(lane >> 1 == iota((half, 2 * half), 0), 0.25, 0.0).astype(BF16)
    rows = MEL_ROWS
    wide = pre_two.shape[1]
    frame_dev = wide - RIM
    usable = masks[0:1]
    total = masks[3:4, 0:1]
    sums = jnp.sum(recv[...], axis=0, keepdims=True)
    mean = to_column(sums, chan) / total
    inv = lax.rsqrt(to_column(sums, chan, chan) / total - mean * mean + 1e-05)
    lane = iota((chan, 128), 1)
    stats[0:chan] = jnp.where(lane == 0, mean, jnp.where(lane == 1, inv, 0.0))
    stats[chan : chan + 8] = jnp.broadcast_to(to_lanes(inv), (8, 128))
    scale = 0.5 * to_column(params[2:3], chan) * inv
    shift = jnp.broadcast_to(0.5 * to_column(params[3:4], chan) - mean * scale, (chan, wide))
    scale = jnp.broadcast_to(scale, (chan, wide))
    mean = jnp.broadcast_to(mean, (chan, frame_dev))
    inv = jnp.broadcast_to(inv, (chan, frame_dev))
    first = jnp.zeros((chan, 128), F32)
    second = jnp.zeros((chan, 128), F32)
    own_mask = usable[:, :frame_dev]
    right[3 * chan :] = jnp.ones((16, rows * frame_dev), BF16)
    table = jnp.zeros((9 * chan, 3 * chan + 16), F32)
    stores = []
    for q in list(range(2, rows + 2)) + [0, 1, rows + 2, rows + 3]:
        r = q // 2
        at = slice(q * chan, (q + 1) * chan)
        m = q - 2
        mask = 0.5 * usable if 0 <= m < rows else usable * (0.5 * row_valid(m, rows))
        if q % 2 == 0:
            if 1 <= r <= rows // 2:
                pooled, at_side = own_rows[(r - 1) * chan : r * chan], (r - 1) * chan
            elif r == 0:
                pooled, at_side = recv_mel[jnp.maximum(me_m - 1, 0), 2 * rows :], rows // 2 * chan
            else:
                pooled, at_side = recv_mel[jnp.minimum(me_m + 1, n_mel - 1), 2 * rows :], (rows // 2 + 1) * chan
            up = jnp.concatenate([dot(pooled, spread), sides[at_side : at_side + chan, :]], axis=1)
        pre = pre_two[at, :]
        value, slope = silu_halves(pre * scale + shift)
        g = up * slope * mask
        grad[at, :] = g
        if not 0 <= m < rows:
            continue
        g = g[:, :frame_dev]
        normed = (pre[:, :frame_dev] - mean) * inv
        first = first + halves(g * normed)
        second = second + halves(g)
        value = value[:, :frame_dev] * own_mask
        both = value if q % 2 == 0 else both + value
        if q % 2:
            pairs[(r - 1) * chan : r * chan, :] = both
            if r % 2 == 0:
                part = pl.ds((r - 2) * chan, 2 * chan)
                stores.append(pltpu.make_async_copy(pairs.at[part, :], pairs_hbm.at[part, :], sems.at[r // 2 - 1]))
                stores[-1].start()
        lanes = slice(m * frame_dev, (m + 1) * frame_dev)
        high = lax.reduce_precision(g, 8, 7)
        right[0:chan, lanes] = high.astype(BF16)
        right[chan : 2 * chan, lanes] = (g - high).astype(BF16)
        right[2 * chan : 3 * chan, lanes] = normed.astype(BF16)
        if m % 4 == 3:
            left = [act[(n + 2) * 3 * chan : (n + 5) * 3 * chan, :frame_dev] for n in range(m - 3, m + 1)]
            lanes = slice((m - 3) * frame_dev, (m + 1) * frame_dev)
            table = table + dot(jnp.concatenate(left, axis=1), right[:, lanes], ((1,), (1,)))
    first = jnp.sum(first, axis=1, keepdims=True)
    second = jnp.sum(second, axis=1, keepdims=True)
    totals = to_lanes(first) + to_lanes(second, chan)
    devices = recv.shape[0]
    block = payload.shape[0] // devices
    payload[pl.ds(0, devices, stride=block), :] = jnp.broadcast_to(totals, (devices, 128))
    both = jnp.concatenate([table[:, :chan] + table[:, chan : 2 * chan], table[:, 2 * chan : 3 * chan]], axis=1)
    single = table[:, 3 * chan : 3 * chan + 1]
    lane = iota((devices, 128), 1)
    constants = jnp.zeros((devices, 128), F32)
    for k in range(block - 2):
        cut, ones = both[k * devices : (k + 1) * devices], single[k * devices : (k + 1) * devices]
        short = devices - cut.shape[0]
        if short:
            cut = jnp.concatenate([cut, jnp.zeros((short, 128), F32)], axis=0)
            ones = jnp.concatenate([ones, jnp.zeros((short, 1), F32)], axis=0)
        payload[pl.ds(1 + k, devices, stride=block), :] = cut
        constants = jnp.where(lane == k, ones, constants)
    payload[pl.ds(block - 1, devices, stride=block), :] = constants
    for store in stores:
        store.wait()


def pool(after, pairs_hbm, out, temp, pairs, sem):
    del after
    load = pltpu.make_async_copy(pairs_hbm, pairs, sem)
    load.start()
    chan, rows, half = out.shape[1:]
    to_mean = jnp.where(iota((2 * half, half), 0) >> 1 == iota((2 * half, half), 1), 0.25, 0.0)
    load.wait()
    pooled = dot(pairs[...], to_mean, precision=EXACT)
    for r in range(rows):
        temp[pl.ds(r, chan, stride=rows), :] = pooled[r * chan : (r + 1) * chan]
    out[0] = temp[...].reshape(chan, rows, half).astype(BF16)


def backward(recv, pre_two, grad, stats_two, w1, x3, stats, params, masks, wb_hbm,
             out, payload, gain_out, bias_out, g3, pre_one, g1, wb, sem):
    fetch = pltpu.make_async_copy(wb_hbm, wb, sem)
    fetch.start()
    chan = params.shape[1]
    rows = MEL_ROWS
    wide = pre_two.shape[1]
    frame_dev = wide - RIM
    usable = masks[0:1]
    behind, ahead = (masks[n : n + 1].astype(BF16) for n in (1, 2))
    total = masks[3:4, 0:1]
    devices = payload.shape[0] // 14
    block = recv.shape[0] // devices
    pre_one[...] = dot(w1[2 * chan : (rows + 4) * chan], x3[...])

    def summed(k):
        return jnp.sum(recv[pl.ds(k, devices, stride=block), :], axis=0, keepdims=True)

    sums = summed(0)
    gain_sum, bias_sum = sums[:, :chan], sums[:, chan:]
    gain_out[...] = gain_sum
    bias_out[...] = bias_sum
    mean, inv = stats_two[0:chan, 0:1], stats_two[0:chan, 1:2]
    factor = to_column(params[2:3], chan) * inv
    gain_part = factor * (to_column(sums, chan) / total * inv)
    bias_part = factor * (to_column(sums, chan, chan) / total) - mean * gain_part
    gain_part = jnp.broadcast_to(gain_part, (chan, wide))
    bias_part = jnp.broadcast_to(bias_part, (chan, wide))
    factor = jnp.broadcast_to(factor, (chan, wide))
    scale = jnp.broadcast_to(stats[chan + 16 :, 0:1], (chan, wide))
    shift = jnp.broadcast_to(stats[chan + 16 :, 1:2], (chan, wide))
    factor_one = jnp.broadcast_to(to_column(params[0:1], chan) * stats[0:chan, 1:2], (chan, wide))
    count = pre_two.shape[0] // chan
    table = jnp.zeros((chan, 128), F32)
    for q in range(count):
        at = slice(q * chan, (q + 1) * chan)
        mask = usable if 0 <= q - 2 < rows else usable * row_valid(q - 2, rows)
        low = (factor * grad[at, :] - (bias_part + pre_two[at, :] * gain_part) * mask).astype(BF16)
        base = q * 3 * chan
        g3[base : base + chan, :], g3[base + 2 * chan : base + 3 * chan, :] = shifted_frames(low, behind, ahead)
        g3[base + chan : base + 2 * chan, :] = low
        if q == 5:
            fetch.wait()
            share = block - 2
            mine = jnp.concatenate([summed(1 + k) for k in range(share)], axis=0)
            single = to_column(summed(block - 1), share)
            factor_l = params[2:3] * stats_two[chan : chan + 1, :chan]
            mine = mine[:, :chan] - (bias_sum * single + gain_sum * mine[:, chan:]) / total
            mine = factor_l * mine
            lower = -(-share // 2)
            mine = jnp.concatenate([mine] + [jnp.zeros((2 * lower - share, chan), F32)] * (share % 2), axis=0)
            mine = jnp.concatenate([mine[:lower], mine[lower:]], axis=1)
            if lower < 9:
                mine = jnp.concatenate([mine, jnp.zeros((9 - lower, 128), F32)], axis=0)
        if q < count - 1 and (q < 5 or (q - 5) % 4):
            continue
        start = 4 * ((q - 2) // 4)
        step = min(4, rows + 2 - start)
        result = dot(
            wb[: step * chan, : (step + 2) * 3 * chan], g3[start * 3 * chan : (start + step + 2) * 3 * chan, :]
        )
        for n in range(step):
            m = start + n - 1
            at = slice((m + 1) * chan, (m + 2) * chan)
            _, slope = silu_halves(pre_one[at, :] * scale + shift)
            mask = 0.5 * usable if 0 <= m < rows else usable * (0.5 * row_valid(m, rows))
            value = result[n * chan : (n + 1) * chan] * slope * mask
            out[at, :] = (value * factor_one).astype(BF16)
            if not 0 <= m < rows:
                continue
            g1[m * chan : (m + 1) * chan, :] = value[:, :frame_dev]
            if m % 4 == 3:
                part = g1[(m - 3) * chan : (m + 1) * chan, :]
                high = lax.reduce_precision(part, 8, 7)
                low = (part - high).astype(BF16)
                taps_in = x3[:, :frame_dev]
                products = dot(high.astype(BF16), taps_in, ((1,), (1,))) + dot(low, taps_in, ((1,), (1,)))
                for k in range(4):
                    table = table + pltpu.roll(products[k * chan : (k + 1) * chan], 128 - (m + k), 1)
    tap = iota((16, 128), 0)
    lane = iota((16, 128), 1)
    i = (tap * 11) >> 5
    select = ((lane == BAND * (tap - 3 * i) + i) & (tap < 9)) | ((lane == 3 * BAND) & (tap == 9))
    rows10 = dot(select.astype(F32), table, ((1,), (1,)), EXACT)
    sums = jnp.concatenate([rows10[0:5], rows10[5:10]], axis=1)
    block = jnp.concatenate([sums, mine], axis=0)
    for d in range(devices):
        payload[14 * d : 14 * (d + 1), :] = block


def transposed(low, w1, x3, stats, masks, ws_hbm, first, normed, ws, pre_one, sem):
    load = pltpu.make_async_copy(ws_hbm, ws, sem)
    load.start()
    chan = low.shape[0] // (MEL_ROWS + 2)
    wide = low.shape[1]
    pre_one[...] = dot(w1[2 * chan : (MEL_ROWS + 4) * chan], x3[...])
    mean = jnp.broadcast_to(stats[0:chan, 0:1], (chan, wide))
    inv = jnp.broadcast_to(stats[0:chan, 1:2], (chan, wide))
    for q in range(MEL_ROWS + 2):
        at = slice(q * chan, (q + 1) * chan)
        mask = masks[0:1] * row_valid(q - 1, MEL_ROWS)
        normed[at, :] = ((pre_one[at, :] - mean) * inv * mask).astype(BF16)
    load.wait()
    first[...] = dot(ws[...], low[...])


def finish(recv, features, stats, k1t, first, normed, ws, params, masks,
           spec_hbm, kernel_one_hbm, kernel_two_hbm, gain_hbm, bias_hbm,
           table, spec_grad, kernel_one, kernel_two, gain_out, bias_out, sems):
    chan = params.shape[1]
    rows = MEL_ROWS
    wide = normed.shape[1]
    frame_dev = wide - RIM
    usable, behind, ahead = (masks[n : n + 1] for n in range(3))
    total = masks[3:4, 0:1]
    gain = params[0:1]
    count = recv.shape[0] // 14
    share = -(-9 * chan // count)
    sums = recv[0:5, :]
    for d in range(1, count):
        sums = sums + recv[14 * d : 14 * d + 5, :]
    ten = jnp.concatenate([sums[:, :chan], sums[:, chan:]], axis=0)
    bias_sum = ten[9:10]
    mean_l, inv_l = stats[chan : chan + 1, :chan], stats[chan + 8 : chan + 9, :chan]
    ten = ten - features[1:2, 0:1] * bias_sum
    k = k1t[0:9]
    gain_sum = inv_l * (jnp.sum(k * ten[0:9], axis=0, keepdims=True) - mean_l * bias_sum)
    gain_out[...] = gain_sum
    bias_out[...] = bias_sum
    stores = [
        pltpu.make_async_copy(gain_out, gain_hbm, sems.at[0]),
        pltpu.make_async_copy(bias_out, bias_hbm, sems.at[1]),
    ]
    stores[0].start()
    stores[1].start()
    factor_l = gain * inv_l
    scale = factor_l * gain_sum / total
    scale = jnp.concatenate([scale, scale], axis=1)
    scale = jnp.concatenate([scale] * ((rows + 2) // 2), axis=1)
    taps = first[...] - dot((ws[...].astype(F32) * scale).astype(BF16), normed[...])
    for part in range(wide // 128):
        table[part] = taps[:, 128 * part : 128 * (part + 1)]
    moved = [
        jnp.concatenate([table[part, pl.ds(b, rows, stride=8), :] for part in range(wide // 128)], axis=1)
        for b in range(3)
    ]
    constant = jnp.sum(k * (factor_l * bias_sum / total), axis=1, keepdims=True)
    for a in range(3):
        row = iota((rows, 1), 0) + (a - 1) + lax.axis_index("mel") * rows
        valid = ((row >= 0) & (row < lax.axis_size("mel") * rows)).astype(F32) * usable
        for b in range(3):
            t = 3 * (2 - a) + 2 - b
            moved[b] = moved[b] - constant[t : t + 1] * valid
    result = pltpu.roll(moved[0], 1, 1) * behind + moved[1] + pltpu.roll(moved[2], wide - 1, 1) * ahead
    spec_grad[0] = (result * usable)[:, :frame_dev]
    stores.append(pltpu.make_async_copy(spec_grad, spec_hbm, sems.at[2]))
    stores[-1].start()
    lower = -(-share // 2)
    left = [recv[pl.ds(5 + p, count, stride=14), :] for p in range(lower)]
    whole = jnp.concatenate([v[:, :chan] for v in left] + [v[:, chan:] for v in left], axis=0)
    for t in range(9):
        kernel_two[t] = whole[t * chan : (t + 1) * chan].T
    stores.append(pltpu.make_async_copy(kernel_two, kernel_two_hbm, sems.at[3]))
    stores[-1].start()
    row = features[0:1, :]
    lane = iota((1, 128), 1)
    gram = jnp.concatenate(
        [jnp.where(lane < 9, pltpu.roll(row, 128 - 9 * t, 1) if t else row, 0.0) for t in range(9)]
        + [jnp.zeros((7, 128), F32)],
        axis=0,
    )
    single = to_column(row, 16, 81)[0:9]
    k_rows = jnp.concatenate([k1t[...], jnp.zeros((112, chan), F32)], axis=0)
    normed_taps = inv_l * (dot(gram, k_rows, precision=EXACT)[0:9] - single * mean_l)
    grad_taps = factor_l * (ten[0:9] - (bias_sum * single + gain_sum * normed_taps) / total)
    for i in range(3):
        kernel_one[i] = grad_taps[3 * i : 3 * i + 3]
    stores.append(pltpu.make_async_copy(kernel_one, kernel_one_hbm, sems.at[4]))
    stores[-1].start()
    for store in stores:
        store.wait()


def run(kernel, outs, scratch, *args, hbm=0, apart=(), flops=10**8, size=4 * 10**6):
    vmem = pl.BlockSpec(memory_space=pltpu.VMEM)
    specs = []
    args = list(args)
    for n, a in enumerate(args):
        if hbm and n >= len(args) - hbm:
            specs.append(pl.BlockSpec(memory_space=pltpu.HBM))
            args[n] = pltpu.with_memory_space_constraint(a, pltpu.HBM)
        else:
            specs.append(vmem)
            args[n] = pltpu.with_memory_space_constraint(a, pltpu.VMEM)
    return pl.pallas_call(
        kernel,
        out_shape=outs,
        in_specs=specs,
        out_specs=[pl.BlockSpec(memory_space=pltpu.HBM) if n in apart else vmem for n in range(len(outs))],
        scratch_shapes=scratch,
        compiler_params=pltpu.CompilerParams(vmem_limit_bytes=30 * 2**20),
        cost_estimate=pl.CostEstimate(flops=flops, bytes_accessed=size, transcendentals=0),
    )(*args)


def shape(dims, dtype=F32):
    return jax.ShapeDtypeStruct(dims, dtype)


def kept(dims, dtype=F32):
    return pltpu.VMEM(dims, dtype)


def far(dims, dtype=F32):
    return pltpu.HBM(dims, dtype)


def exchange(blocks, axes=AXES):
    return lax.all_to_all(blocks, axes, 0, 0, tiled=True)


def exchange_rows(rows, axes=AXES):
    return exchange(rows[:, None, :], axes)[:, 0, :]


def shards(spectrum, clip_bounds, kernel_one, gain_one, bias_one, kernel_two, gain_two, bias_two, pooled_grad):
    _, rows, frame_dev = spectrum.shape
    chan = kernel_two.shape[0]
    n_mel, n_tm = lax.axis_size("mel"), lax.axis_size("tm")
    devices = n_mel * n_tm
    half = frame_dev // 2
    wide = frame_dev + RIM
    mels = n_mel * rows

    packed, own = run(
        pack_mel,
        [kept((n_mel, 2 * rows + chan, half), BF16), kept(pooled_grad.shape, BF16)],
        [
            pltpu.VMEM(spectrum.shape, BF16),
            pltpu.SemaphoreType.DMA((2,)),
        ],
        spectrum,
        pooled_grad,
        hbm=2,
    )
    recv_mel = exchange(packed, "mel")
    ext = rows + 6
    span = 6 * 3 * chan
    wf, wb, w1, ws, pairs, singles, k1t, params, masks, edge_masks, twice, own_rows = run(
        weights,
        [
            kept((4 * chan, span), BF16),
            far((4 * chan, span), BF16),
            kept((ext * chan, 128), BF16),
            far((rows * 8, (rows + 2) * chan), BF16),
            kept((chan, 128)),
            kept((chan, 128)),
            kept((16, chan)),
            kept((8, chan)),
            kept((8, wide)),
            kept((n_tm * 8, 128)),
            kept((128, 128)),
            kept((chan * rows // 2, half), BF16),
        ],
        [
            pltpu.VMEM((9, chan, chan), BF16),
            pltpu.VMEM((3, 3, chan), BF16),
            pltpu.VMEM((4, 1, chan), F32),
            pltpu.SMEM(clip_bounds.shape, jnp.int32),
            pltpu.VMEM((4 * chan, span), BF16),
            pltpu.VMEM((rows * 8, (rows + 2) * chan), BF16),
            pltpu.VMEM((chan * rows // 2, half), F32),
            pltpu.SemaphoreType.DMA((9,)),
        ],
        own,
        clip_bounds,
        jnp.transpose(kernel_two, (2, 3, 0, 1)).reshape(9, chan, chan),
        jnp.transpose(kernel_one, (1, 2, 0)),
        gain_one[None],
        bias_one[None],
        gain_two[None],
        bias_two[None],
        hbm=7,
        apart=(1, 3),
    )
    (packed,) = run(
        pack_tm,
        [kept((n_tm, 16, 128), BF16)],
        [pltpu.VMEM((n_tm * 16, 128), F32)],
        recv_mel,
        own_rows,
        masks,
    )
    recv_tm = exchange(packed, "tm")
    pre_two, payload, act, x3, stats_one, features = run(
        forward_one,
        [
            kept(((rows + 4) * chan, wide)),
            kept((devices, 128)),
            kept((ext * 3 * chan, wide), BF16),
            kept((128, wide), BF16),
            kept((2 * chan + 16, 128)),
            kept((8, 128)),
        ],
        [pltpu.VMEM((ext * chan, wide), F32), pltpu.VMEM((mels + 8, wide), F32)],
        recv_mel,
        recv_tm,
        pairs,
        singles,
        twice,
        w1,
        wf,
        params,
        masks,
        edge_masks,
    )
    recv = exchange_rows(payload)
    grad, payload, row_pairs, stats_two = run(
        backward_scaled,
        [
            kept(((rows + 4) * chan, wide)),
            kept((devices * sum_rows(devices, 9 * chan), 128)),
            far((rows // 2 * chan, frame_dev)),
            kept((chan + 8, 128)),
        ],
        [
            pltpu.VMEM(((rows // 2 + 2) * chan, RIM), F32),
            pltpu.VMEM((rows // 2 * chan, frame_dev), F32),
            pltpu.VMEM((3 * chan + 16, rows * frame_dev), BF16),
            pltpu.SemaphoreType.DMA((rows // 4,)),
        ],
        recv,
        pre_two,
        act,
        recv_mel,
        recv_tm,
        own_rows,
        params,
        masks,
        apart=(2,),
    )
    recv = exchange_rows(payload)
    low, payload, gain_two_grad, bias_two_grad = run(
        backward,
        [
            kept(((rows + 2) * chan, wide), BF16),
            kept((devices * 14, 128)),
            shape((1, chan)),
            shape((1, chan)),
        ],
        [
            pltpu.VMEM(((rows + 4) * 3 * chan, wide), BF16),
            pltpu.VMEM(((rows + 2) * chan, wide), F32),
            pltpu.VMEM((rows * chan, frame_dev), F32),
            pltpu.VMEM((4 * chan, span), BF16),
            pltpu.SemaphoreType.DMA,
        ],
        recv,
        pre_two,
        grad,
        stats_two,
        w1,
        x3,
        stats_one,
        params,
        masks,
        wb,
        hbm=1,
    )
    recv = exchange_rows(payload)
    (pooled,) = run(
        pool,
        [shape((1, chan, rows // 2, half), BF16)],
        [
            pltpu.VMEM((rows // 2 * chan, 128), F32),
            pltpu.VMEM((rows // 2 * chan, frame_dev), F32),
            pltpu.SemaphoreType.DMA,
        ],
        payload,
        row_pairs,
        hbm=1,
    )
    first, normed, ws = run(
        transposed,
        [
            kept((rows * 8, wide)),
            kept(((rows + 2) * chan, wide), BF16),
            kept((rows * 8, (rows + 2) * chan), BF16),
        ],
        [pltpu.VMEM(((rows + 2) * chan, wide), F32), pltpu.SemaphoreType.DMA],
        low,
        w1,
        x3,
        stats_one,
        masks,
        ws,
        hbm=1,
    )
    spec_grad, kernel_one_grad, kernel_two_grad, gain_one_grad, bias_one_grad = run(
        finish,
        [
            shape((1, rows, frame_dev)),
            shape((3, 3, chan)),
            shape((9, chan, chan)),
            shape((1, chan)),
            shape((1, chan)),
        ],
        [
            pltpu.VMEM((3, rows * 8, 128), F32),
            pltpu.VMEM((1, rows, frame_dev), F32),
            pltpu.VMEM((3, 3, chan), F32),
            pltpu.VMEM((9, chan, chan), F32),
            pltpu.VMEM((1, chan), F32),
            pltpu.VMEM((1, chan), F32),
            pltpu.SemaphoreType.DMA((5,)),
        ],
        recv,
        features,
        stats_one,
        k1t,
        first,
        normed,
        ws,
        params,
        masks,
        apart=range(5),
    )
    kernel_two_grad = jnp.transpose(kernel_two_grad.reshape(3, 3, chan, chan), (2, 3, 0, 1))
    return (
        pooled,
        spec_grad,
        jnp.transpose(kernel_one_grad, (2, 0, 1)),
        gain_one_grad[0],
        bias_one_grad[0],
        kernel_two_grad,
        gain_two_grad[0],
        bias_two_grad[0],
    )


def solution(mesh):
    return jax.shard_map(
        shards,
        mesh=mesh,
        in_specs=(
            P(None, "mel", "tm"),
            P(),
            P(),
            P(),
            P(),
            P(),
            P(),
            P(),
            P(None, None, "mel", "tm"),
        ),
        out_specs=(P(None, None, "mel", "tm"), P(None, "mel", "tm"), P(), P(), P(), P(), P(), P()),
        check_vma=False,
    )
```

```python
import functools

import jax
import jax.numpy as jnp
from jax import lax
from jax.experimental import pallas as pl
from jax.experimental.pallas import tpu as pltpu
from jax.sharding import PartitionSpec as P

F32 = jnp.float32
BF16 = jnp.bfloat16
AXES = ("mel", "tm")
EXACT = lax.Precision.HIGHEST
RIM = 128
BAND = 24
MEL_ROWS = 16


def iota(shape, dim):
    return lax.broadcasted_iota(jnp.int32, shape, dim)


def dot(a, b, over=((1,), (0,)), precision=None):
    return lax.dot_general(a, b, (over, ((), ())), precision=precision, preferred_element_type=F32)


def to_column(lanes, count, start=0):
    shape = (count, lanes.shape[1])
    return jnp.sum(jnp.where(iota(shape, 1) == iota(shape, 0) + start, lanes, 0.0), axis=1, keepdims=True)


def to_lanes(column, start=0, width=128):
    shape = (column.shape[0], width)
    return jnp.sum(jnp.where(iota(shape, 1) == iota(shape, 0) + start, column, 0.0), axis=0, keepdims=True)


def halves(v):
    return sum(v[:, n : n + 128] for n in range(128, v.shape[1], 128)) + v[:, :128]


def frame_masks(bounds, frames):
    last = bounds.shape[1] - 1

    def living(f):
        return (f >= 0) & (f < bounds[0, last])

    def paired(f):
        both = living(f) & living(f + 1)
        for k in range(1, last):
            both = both & (f + 1 != bounds[0, k])
        return both

    return tuple(m.astype(F32) for m in (living(frames), paired(frames - 1), paired(frames)))


def row_valid(row, rows):
    mel = lax.axis_index("mel") * rows + row
    return ((mel >= 0) & (mel < lax.axis_size("mel") * rows)).astype(F32)


def start_all(*pairs, sems):
    copies = [pltpu.make_async_copy(src, dst, sems.at[n]) for n, (src, dst) in enumerate(pairs)]
    for copy in copies:
        copy.start()
    return copies


def wait_all(copies):
    for copy in copies:
        copy.wait()


def shifted_frames(value, behind, ahead):
    wide = value.shape[1]
    return pltpu.roll(value, 1, 1) * behind, pltpu.roll(value, wide - 1, 1) * ahead


def pack_mel(spec_hbm, grad_hbm, out, own, spec, sems):
    wait_all(start_all((spec_hbm, spec), (grad_hbm, own), sems=sems))
    me = lax.axis_index("mel")
    x = spec[0]
    rows, frame_dev = x.shape
    half = frame_dev // 2
    g = own[0].astype(F32)
    top = g[:, 0, :]
    bottom = g[:, g.shape[1] - 1, :]
    for j in range(out.shape[0]):
        out[j, 0:rows] = x[:, :half]
        out[j, rows : 2 * rows] = x[:, half:]
        edge = jnp.where(j == me - 1, top, 0.0) + jnp.where(j == me + 1, bottom, 0.0)
        out[j, 2 * rows :] = edge.astype(BF16)


def weights(own, bounds_hbm, k2_hbm, k1_hbm, gain_one_hbm, bias_one_hbm, gain_two_hbm, bias_two_hbm,
            wf, wb, w1, ws_hbm, pairs, singles, k1t, params, masks, edge_masks, twice, own_rows,
            k2, k1, vectors, bounds, ws, temp, sems):
    loads = start_all(
        (bounds_hbm, bounds),
        (k2_hbm, k2),
        (k1_hbm, k1),
        (gain_one_hbm, vectors.at[0]),
        (bias_one_hbm, vectors.at[1]),
        (gain_two_hbm, vectors.at[2]),
        (bias_two_hbm, vectors.at[3]),
        sems=sems,
    )
    _, many, count, half = own.shape
    temp[...] = own[0].astype(F32).reshape(many * count, half)
    for r in range(count):
        own_rows[r * many : (r + 1) * many] = temp[pl.ds(r, many, stride=count), :].astype(BF16)
    wait_all(loads)
    chan = k2.shape[1]
    span = wf.shape[1]
    taps = [k2[t].astype(F32) for t in range(9)]
    rest = jnp.zeros((chan, span - 9 * chan), F32)
    forward = jnp.concatenate(taps + [rest], axis=1)
    backward = jnp.concatenate([taps[8 - t].T for t in range(9)] + [rest], axis=1)
    for r in range(wb.shape[0] // chan):
        at = slice(r * chan, (r + 1) * chan)
        wb[at] = (pltpu.roll(backward, 3 * chan * r, 1) if r else backward).astype(BF16)
    full = jnp.concatenate([k1[n].astype(F32) for n in range(3)] + [jnp.zeros((7, chan), F32)], axis=0)
    low = [
        jnp.concatenate([full[3 * (2 - a) + 2 - b : 3 * (2 - a) + 3 - b] for a in range(3)], axis=1)
        for b in range(3)
    ]
    base = jnp.concatenate(low + [jnp.zeros((5, 3 * chan), F32)], axis=0)
    base = jnp.concatenate([base, jnp.zeros((8, ws.shape[1] - 3 * chan), F32)], axis=1)
    for m in range(ws.shape[0] // 8):
        ws[8 * m : 8 * m + 8] = (pltpu.roll(base, chan * m, 1) if m else base).astype(BF16)
    store_ws = pltpu.make_async_copy(ws, ws_hbm, sems.at[7])
    store_ws.start()
    wide = masks.shape[1]
    frame_dev = wide - RIM
    lane = iota((1, wide), 1)
    frames = lax.axis_index("tm") * frame_dev + jnp.where(lane < frame_dev + RIM // 2, lane, lane - wide)
    last = bounds.shape[1] - 1
    pixels = (bounds[0, last] * (lax.axis_size("mel") * MEL_ROWS)).astype(F32)
    masks[...] = jnp.concatenate(
        list(frame_masks(bounds, frames)) + [jnp.full((1, wide), 1.0) * pixels, jnp.zeros((4, wide), F32)], axis=0
    )
    q = iota(edge_masks.shape, 0)
    lane = iota(edge_masks.shape, 1)
    k = q % 8
    frames = (q // 8) * frame_dev + jnp.where(k < 4, k, k + frame_dev - 8)
    living, behind, ahead = frame_masks(bounds, frames)
    living = jnp.where((k == 0) | (k == 7), living, 0.0)
    edge_masks[...] = jnp.where(lane == 0, living, jnp.where(lane == 1, behind, jnp.where(lane == 2, ahead, 0.0)))
    params[...] = jnp.concatenate(
        [vectors[n] for n in range(4)] + [jnp.zeros((4, chan), F32)], axis=0
    )
    tap = iota((16, 128), 0)
    lane = iota((16, 128), 1)
    i = (tap * 11) >> 5
    ninth = (lane * 57) >> 9
    to_band = (lane == BAND * (tap - 3 * i) + i) & (tap < 9)
    to_left = (ninth == tap) & (tap < 9)
    to_right = (lane - 9 * ninth == tap) & (lane < 81)
    to_single = (lane == 81 + tap) & (tap < 9)
    source = iota((128, 128), 0) - 81
    lane = iota((128, 128), 1)
    ninth = (lane * 57) >> 9
    inside = (source >= 0) & (source < 9) & (lane < 81)
    twice[...] = jnp.where(inside, (source == ninth).astype(F32) + (source == lane - 9 * ninth).astype(F32), 0.0)
    for r in range(wf.shape[0] // chan):
        at = slice(r * chan, (r + 1) * chan)
        wf[at] = (pltpu.roll(forward, 3 * chan * r, 1) if r else forward).astype(BF16)
    k1t[...] = full
    k = full.astype(BF16)
    lanes = [dot(k, select.astype(BF16), ((0,), (0,))) for select in (to_band, to_left, to_right, to_single)]
    pairs[...] = lanes[1] * lanes[2]
    singles[...] = lanes[3]
    for m in range(w1.shape[0] // chan):
        w1[m * chan : (m + 1) * chan] = (pltpu.roll(lanes[0], m, 1) if m else lanes[0]).astype(BF16)
    store_ws.wait()


def feature_rows(shifted, axis_shift, weight, centre):
    z = [None] * 9
    for j in range(3):
        for i in range(3):
            z[3 * i + j] = axis_shift(shifted[j], i) - centre

    def folded(v):
        if v.shape[1] > 128:
            v = v[:, :128] + v[:, 128:]
        return jnp.sum(v, axis=0, keepdims=True)

    rows = [None] * 96
    for s in range(9):
        left = z[s] * weight
        rows[81 + s] = folded(left)
        for t in range(s, 9):
            rows[9 * s + t] = rows[9 * t + s] = folded(left * z[t])
    zero = jnp.zeros((1, 128), F32)
    stack = jnp.concatenate([zero if r is None else r for r in rows], axis=0)
    return to_lanes(jnp.sum(stack, axis=1, keepdims=True))


def pack_tm(recv, own_rows, masks, out, spread):
    count = out.shape[0]
    n_mel = recv.shape[0]
    me_m, me_t = lax.axis_index("mel"), lax.axis_index("tm")
    rows = MEL_ROWS
    half = recv.shape[2]
    frame_dev = 2 * half
    mels = n_mel * rows
    lane = iota((1, frame_dev), 1)
    usable, behind, ahead = (masks[n : n + 1, :frame_dev] for n in range(3))
    x = jnp.concatenate(
        [
            jnp.concatenate([recv[j, 0:rows] for j in range(n_mel)], axis=0),
            jnp.concatenate([recv[j, rows : 2 * rows] for j in range(n_mel)], axis=0),
        ],
        axis=1,
    )
    x = x.astype(F32) * usable
    inner = jnp.where((lane > 0) & (lane < frame_dev - 1), usable, 0.0)
    number = mels * jnp.sum(inner, axis=1, keepdims=True)
    centre = jnp.sum(jnp.sum(x, axis=0, keepdims=True), axis=1, keepdims=True)
    centre = centre / (mels * jnp.maximum(jnp.sum(usable, axis=1, keepdims=True), 1.0))
    centre = lax.reduce_precision(centre, 8, 7)
    row = iota((mels, frame_dev), 0)

    def mel_shift(v, i):
        if i == 1:
            return v
        if i == 0:
            return jnp.where(row == 0, 0.0, pltpu.roll(v, 1, 0))
        return jnp.where(row == mels - 1, 0.0, pltpu.roll(v, mels - 1, 0))

    shifted = [pltpu.roll(x, 1, 1) * behind, x, pltpu.roll(x, frame_dev - 1, 1) * ahead]
    features = feature_rows(shifted, mel_shift, inner, centre)
    lane = iota((1, 128), 1)
    features = jnp.where(lane == 90, centre, jnp.where(lane == 91, number, features))
    high = lax.reduce_precision(features, 8, 7)
    mid = lax.reduce_precision(features - high, 8, 7)
    low = features - high - mid
    pick = iota((8, frame_dev), 0)
    column = jnp.where(pick < 4, pick, frame_dev - 8 + pick)
    edges = dot((iota((8, frame_dev), 1) == column).astype(BF16), x.astype(BF16), ((1,), (1,)))
    edges = jnp.concatenate([edges, jnp.zeros((8, 128 - mels), F32)], axis=1)
    target = iota((count, half), 0)
    at = iota((count, half), 1)
    choose = ((target == me_t - 1) & (at == 0)) | ((target == me_t + 1) & (at == half - 1))
    choose = choose.astype(BF16)
    above = recv[jnp.maximum(me_m - 1, 0), 2 * rows :]
    below = recv[jnp.minimum(me_m + 1, n_mel - 1), 2 * rows :]
    columns = dot(choose, own_rows[...], ((1,), (1,)))
    outer = jnp.concatenate([dot(choose, above, ((1,), (1,))), dot(choose, below, ((1,), (1,)))], axis=1)
    parts = columns.shape[1] // 128
    for q in range(parts):
        spread[pl.ds(8 + q, count, stride=16), :] = columns[:, 128 * q : 128 * (q + 1)]
    spread[pl.ds(8 + parts, count, stride=16), :] = outer
    common = jnp.concatenate([high, mid, low], axis=0)
    for j in range(count):
        tail = jnp.concatenate([spread[16 * j + 8 : 16 * j + 13, :], common], axis=0)
        out[j] = jnp.concatenate([edges, tail], axis=0).astype(BF16)


def side_columns(recv_tm, out):
    me_t = lax.axis_index("tm")
    count = recv_tm.shape[0]
    after = recv_tm[jnp.minimum(me_t + 1, count - 1)].astype(F32)
    before = recv_tm[jnp.maximum(me_t - 1, 0)].astype(F32)
    after = jnp.concatenate([after[8 + q : 9 + q] for q in range(5)], axis=1)
    before = jnp.concatenate([before[8 + q : 9 + q] for q in range(5)], axis=1)
    side = iota((16, after.shape[1]), 0)
    sides = jnp.where(side == 0, after, jnp.where(side == 1, before, 0.0)).astype(BF16)
    lane = iota((16, RIM), 1)
    side = iota((16, RIM), 0)
    columns = ((side == 0) & (lane < 2)) | ((side == 1) & (lane >= RIM - 2))
    out[...] = dot(sides, jnp.where(columns, 0.25, 0.0).astype(BF16), ((0,), (0,)))


def silu_halves(h):
    t = jnp.tanh(h)
    one = 1.0 + t
    return h * one, one * (1.0 + h * (1.0 - t))


def forward_one(recv_mel, recv_tm, pairs, singles, twice, w1, wf, params, masks, edge_masks,
                pre_two, payload, act, x3, stats, features_out, pre_one, xs):
    n_mel, count = recv_mel.shape[0], recv_tm.shape[0]
    rows = MEL_ROWS
    mels = n_mel * rows
    half = recv_mel.shape[2]
    frame_dev = 2 * half
    wide = frame_dev + RIM
    chan = params.shape[1]
    me_m, me_t = lax.axis_index("mel"), lax.axis_index("tm")
    usable, behind, ahead = (masks[n : n + 1] for n in range(3))
    total = masks[3:4, 0:1]
    x = jnp.concatenate(
        [
            jnp.concatenate([recv_mel[j, 0:rows] for j in range(n_mel)], axis=0),
            jnp.concatenate([recv_mel[j, rows : 2 * rows] for j in range(n_mel)], axis=0),
        ],
        axis=1,
    ).astype(F32)
    after = recv_tm[jnp.minimum(me_t + 1, count - 1)].astype(F32)[0:8, :mels]
    before = recv_tm[jnp.maximum(me_t - 1, 0)].astype(F32)[0:8, :mels]
    after = jnp.where(me_t + 1 < count, after, 0.0)
    before = jnp.where(me_t > 0, before, 0.0)
    sides = jnp.concatenate([after[0:4], before[4:8], jnp.zeros((8, mels), F32)], axis=0).astype(BF16)
    side = iota((16, RIM), 0)
    place = iota((16, RIM), 1) == jnp.where(side < 4, side, jnp.where(side < 8, side + RIM - 8, -1))
    x = jnp.concatenate([x, dot(sides, place.astype(BF16), ((0,), (0,)))], axis=1) * usable
    xs[0:8] = jnp.zeros((8, wide), F32)
    xs[mels : mels + 8] = jnp.zeros((8, wide), F32)
    xs[4 : mels + 4] = x
    near = xs[pl.ds(pl.multiple_of(me_m * rows, 8), BAND), :]
    x3[...] = jnp.concatenate(
        [
            pltpu.roll(near, 1, 1) * behind,
            near,
            pltpu.roll(near, wide - 1, 1) * ahead,
            jnp.broadcast_to(usable, (BAND, wide)),
            jnp.zeros((128 - 4 * BAND, wide), F32),
        ],
        axis=0,
    ).astype(BF16)
    pre_one[...] = dot(w1[...], x3[...])
    parts = [recv_tm[d].astype(F32)[8:16] for d in range(count)]
    parts = [p[5:6] + p[6:7] + p[7:8] for p in parts]
    centres = [p[:, 90:91] for p in parts]
    numbers = [p[:, 91:92] for p in parts]
    weight = functools.reduce(jnp.add, numbers)
    centre = functools.reduce(jnp.add, [c * n for c, n in zip(centres, numbers)]) / jnp.maximum(weight, 1.0)
    lane = iota((1, 128), 1)
    features = jnp.zeros((1, 128), F32)
    moved = jnp.zeros((1, 128), F32)
    for part, c, n in zip(parts, centres, numbers):
        delta = c - centre
        moved = moved + delta * part
        features = features + part + delta * n * jnp.where(lane < 81, delta, 1.0)
    moved = dot(jnp.broadcast_to(moved, (8, 128)), twice[...], precision=EXACT)[0:1]
    features = features + moved
    edge = recv_tm[:, 0:8, :].astype(F32).reshape(count * 8, 128)
    q_usable, q_behind, q_ahead = (edge_masks[:, n : n + 1] for n in range(3))
    lane = iota((count * 8, 128), 1)

    def lane_shift(v, i):
        if i == 1:
            return v
        if i == 0:
            return jnp.where(lane < mels, pltpu.roll(v, 1, 1), 0.0)
        return pltpu.roll(v, 127, 1)

    shifted = [
        pltpu.roll(edge, 1, 0) * q_behind,
        edge,
        pltpu.roll(edge, count * 8 - 1, 0) * q_ahead,
    ]
    features = features + feature_rows(shifted, lane_shift, jnp.where(lane < mels, q_usable, 0.0), centre)
    features = jnp.where(iota((1, 128), 1) < 90, features, 0.0)
    features_out[...] = jnp.concatenate(
        [features, jnp.broadcast_to(centre, (1, 128)), jnp.zeros((6, 128), F32)], axis=0
    )
    near_mean = jnp.sum(singles[...] * features, axis=1, keepdims=True) / total
    square = jnp.sum(pairs[...] * features, axis=1, keepdims=True) / total
    inv = lax.rsqrt(square - near_mean * near_mean + 1e-05)
    mean = near_mean + centre * jnp.sum(singles[...], axis=1, keepdims=True)
    lane = iota((chan, 128), 1)
    stats[0:chan] = jnp.where(lane == 0, mean, jnp.where(lane == 1, inv, 0.0))
    stats[chan : chan + 8] = jnp.broadcast_to(to_lanes(near_mean), (8, 128))
    stats[chan + 8 : chan + 16] = jnp.broadcast_to(to_lanes(inv), (8, 128))
    scale = 0.5 * to_column(params[0:1], chan) * inv
    shift = 0.5 * to_column(params[1:2], chan) - mean * scale
    stats[chan + 16 :] = jnp.where(lane == 0, scale, jnp.where(lane == 1, shift, 0.0))
    scale = jnp.broadcast_to(scale, (chan, wide))
    shift = jnp.broadcast_to(shift, (chan, wide))
    ext = w1.shape[0] // chan
    block, taps = wf.shape
    first = jnp.zeros((chan, 128), F32)
    second = jnp.zeros((chan, 128), F32)
    own_mask = usable[:, :frame_dev]
    low_masks = [m.astype(BF16) for m in (usable, behind, ahead)]
    for r in range(ext):
        value, _ = silu_halves(pre_one[r * chan : (r + 1) * chan, :] * scale + shift)
        if not 0 <= r - 3 < rows:
            value = value * row_valid(r - 3, rows)
        base = r * 3 * chan
        low = value.astype(BF16) * low_masks[0]
        act[base : base + chan, :], act[base + 2 * chan : base + 3 * chan, :] = shifted_frames(low, *low_masks[1:])
        act[base + chan : base + 2 * chan, :] = low
        if r < 3 or r % 2 == 0:
            continue
        g = (r - 3) // 2
        result = dot(wf[...], act[g * 3 * block : g * 3 * block + taps, :])
        pre_two[g * block : (g + 1) * block] = result
        for q in range(2):
            if 2 <= 2 * g + q < rows + 2:
                p = result[q * chan : (q + 1) * chan, :frame_dev]
                masked = p * own_mask
                first = first + halves(masked)
                second = second + halves(masked * p)
    first = jnp.sum(first, axis=1, keepdims=True)
    second = jnp.sum(second, axis=1, keepdims=True)
    payload[...] = jnp.broadcast_to(to_lanes(first) + to_lanes(second, chan), payload.shape)


def sum_rows(devices, taps):
    return -(-taps // devices) + 2


def backward_scaled(recv, pre_two, act, recv_mel, recv_tm, own_rows, params, masks,
                    grad, payload, pairs_hbm, stats, sides, pairs, right, sems):
    side_columns(recv_tm, sides)
    me_m, n_mel = lax.axis_index("mel"), recv_mel.shape[0]
    chan = params.shape[1]
    half = own_rows.shape[1]
    lane = iota((half, 2 * half), 1)
    spread = jnp.where(lane >> 1 == iota((half, 2 * half), 0), 0.25, 0.0).astype(BF16)
    rows = MEL_ROWS
    wide = pre_two.shape[1]
    frame_dev = wide - RIM
    usable = masks[0:1]
    total = masks[3:4, 0:1]
    sums = jnp.sum(recv[...], axis=0, keepdims=True)
    mean = to_column(sums, chan) / total
    inv = lax.rsqrt(to_column(sums, chan, chan) / total - mean * mean + 1e-05)
    lane = iota((chan, 128), 1)
    stats[0:chan] = jnp.where(lane == 0, mean, jnp.where(lane == 1, inv, 0.0))
    stats[chan : chan + 8] = jnp.broadcast_to(to_lanes(inv), (8, 128))
    scale = 0.5 * to_column(params[2:3], chan) * inv
    shift = jnp.broadcast_to(0.5 * to_column(params[3:4], chan) - mean * scale, (chan, wide))
    scale = jnp.broadcast_to(scale, (chan, wide))
    mean = jnp.broadcast_to(mean, (chan, frame_dev))
    inv = jnp.broadcast_to(inv, (chan, frame_dev))
    first = jnp.zeros((chan, 128), F32)
    second = jnp.zeros((chan, 128), F32)
    own_mask = usable[:, :frame_dev]
    right[3 * chan :] = jnp.ones((16, rows * frame_dev), BF16)
    table = jnp.zeros((9 * chan, 3 * chan + 16), F32)
    stores = []
    for q in list(range(2, rows + 2)) + [0, 1, rows + 2, rows + 3]:
        r = q // 2
        at = slice(q * chan, (q + 1) * chan)
        m = q - 2
        mask = 0.5 * usable if 0 <= m < rows else usable * (0.5 * row_valid(m, rows))
        if q % 2 == 0:
            if 1 <= r <= rows // 2:
                pooled, at_side = own_rows[(r - 1) * chan : r * chan], (r - 1) * chan
            elif r == 0:
                pooled, at_side = recv_mel[jnp.maximum(me_m - 1, 0), 2 * rows :], rows // 2 * chan
            else:
                pooled, at_side = recv_mel[jnp.minimum(me_m + 1, n_mel - 1), 2 * rows :], (rows // 2 + 1) * chan
            up = jnp.concatenate([dot(pooled, spread), sides[at_side : at_side + chan, :]], axis=1)
        pre = pre_two[at, :]
        value, slope = silu_halves(pre * scale + shift)
        g = up * slope * mask
        grad[at, :] = g
        if not 0 <= m < rows:
            continue
        g = g[:, :frame_dev]
        normed = (pre[:, :frame_dev] - mean) * inv
        first = first + halves(g * normed)
        second = second + halves(g)
        value = value[:, :frame_dev] * own_mask
        both = value if q % 2 == 0 else both + value
        if q % 2:
            pairs[(r - 1) * chan : r * chan, :] = both
            if r % 2 == 0:
                part = pl.ds((r - 2) * chan, 2 * chan)
                stores.append(pltpu.make_async_copy(pairs.at[part, :], pairs_hbm.at[part, :], sems.at[r // 2 - 1]))
                stores[-1].start()
        lanes = slice(m * frame_dev, (m + 1) * frame_dev)
        high = lax.reduce_precision(g, 8, 7)
        right[0:chan, lanes] = high.astype(BF16)
        right[chan : 2 * chan, lanes] = (g - high).astype(BF16)
        right[2 * chan : 3 * chan, lanes] = normed.astype(BF16)
        if m % 4 == 3:
            left = [act[(n + 2) * 3 * chan : (n + 5) * 3 * chan, :frame_dev] for n in range(m - 3, m + 1)]
            lanes = slice((m - 3) * frame_dev, (m + 1) * frame_dev)
            table = table + dot(jnp.concatenate(left, axis=1), right[:, lanes], ((1,), (1,)))
    first = jnp.sum(first, axis=1, keepdims=True)
    second = jnp.sum(second, axis=1, keepdims=True)
    totals = to_lanes(first) + to_lanes(second, chan)
    devices = recv.shape[0]
    block = payload.shape[0] // devices
    payload[pl.ds(0, devices, stride=block), :] = jnp.broadcast_to(totals, (devices, 128))
    both = jnp.concatenate([table[:, :chan] + table[:, chan : 2 * chan], table[:, 2 * chan : 3 * chan]], axis=1)
    single = table[:, 3 * chan : 3 * chan + 1]
    lane = iota((devices, 128), 1)
    constants = jnp.zeros((devices, 128), F32)
    for k in range(block - 2):
        cut, ones = both[k * devices : (k + 1) * devices], single[k * devices : (k + 1) * devices]
        short = devices - cut.shape[0]
        if short:
            cut = jnp.concatenate([cut, jnp.zeros((short, 128), F32)], axis=0)
            ones = jnp.concatenate([ones, jnp.zeros((short, 1), F32)], axis=0)
        payload[pl.ds(1 + k, devices, stride=block), :] = cut
        constants = jnp.where(lane == k, ones, constants)
    payload[pl.ds(block - 1, devices, stride=block), :] = constants
    for store in stores:
        store.wait()


def pool(after, pairs_hbm, out, temp, pairs, sem):
    del after
    load = pltpu.make_async_copy(pairs_hbm, pairs, sem)
    load.start()
    chan, rows, half = out.shape[1:]
    to_mean = jnp.where(iota((2 * half, half), 0) >> 1 == iota((2 * half, half), 1), 0.25, 0.0)
    load.wait()
    pooled = dot(pairs[...], to_mean, precision=EXACT)
    for r in range(rows):
        temp[pl.ds(r, chan, stride=rows), :] = pooled[r * chan : (r + 1) * chan]
    out[0] = temp[...].reshape(chan, rows, half).astype(BF16)


def backward(recv, pre_two, grad, stats_two, w1, x3, stats, params, masks, wb,
             out, payload, gain_out, bias_out, g3, pre_one, g1):
    chan = params.shape[1]
    rows = MEL_ROWS
    wide = pre_two.shape[1]
    frame_dev = wide - RIM
    usable = masks[0:1]
    behind, ahead = (masks[n : n + 1].astype(BF16) for n in (1, 2))
    total = masks[3:4, 0:1]
    devices = payload.shape[0] // 14
    block = recv.shape[0] // devices
    pre_one[...] = dot(w1[2 * chan : (rows + 4) * chan], x3[...])

    def summed(k):
        return jnp.sum(recv[pl.ds(k, devices, stride=block), :], axis=0, keepdims=True)

    sums = summed(0)
    gain_sum, bias_sum = sums[:, :chan], sums[:, chan:]
    gain_out[...] = gain_sum
    bias_out[...] = bias_sum
    mean, inv = stats_two[0:chan, 0:1], stats_two[0:chan, 1:2]
    factor = to_column(params[2:3], chan) * inv
    gain_part = factor * (to_column(sums, chan) / total * inv)
    bias_part = factor * (to_column(sums, chan, chan) / total) - mean * gain_part
    gain_part = jnp.broadcast_to(gain_part, (chan, wide))
    bias_part = jnp.broadcast_to(bias_part, (chan, wide))
    factor = jnp.broadcast_to(factor, (chan, wide))
    scale = jnp.broadcast_to(stats[chan + 16 :, 0:1], (chan, wide))
    shift = jnp.broadcast_to(stats[chan + 16 :, 1:2], (chan, wide))
    factor_one = jnp.broadcast_to(to_column(params[0:1], chan) * stats[0:chan, 1:2], (chan, wide))
    count = pre_two.shape[0] // chan
    table = jnp.zeros((chan, 128), F32)
    for q in range(count):
        at = slice(q * chan, (q + 1) * chan)
        mask = usable if 0 <= q - 2 < rows else usable * row_valid(q - 2, rows)
        low = (factor * grad[at, :] - (bias_part + pre_two[at, :] * gain_part) * mask).astype(BF16)
        base = q * 3 * chan
        g3[base : base + chan, :], g3[base + 2 * chan : base + 3 * chan, :] = shifted_frames(low, behind, ahead)
        g3[base + chan : base + 2 * chan, :] = low
        if q < 3 or q % 2 == 0:
            continue
        start = q - 3
        result = dot(wb[...], g3[start * 3 * chan : (start + 4) * 3 * chan, :])
        for n in range(2):
            m = start + n - 1
            at = slice((m + 1) * chan, (m + 2) * chan)
            _, slope = silu_halves(pre_one[at, :] * scale + shift)
            mask = 0.5 * usable if 0 <= m < rows else usable * (0.5 * row_valid(m, rows))
            value = result[n * chan : (n + 1) * chan] * slope * mask
            out[at, :] = (value * factor_one).astype(BF16)
            if not 0 <= m < rows:
                continue
            g1[m * chan : (m + 1) * chan, :] = value[:, :frame_dev]
            if m % 4 == 3:
                part = g1[(m - 3) * chan : (m + 1) * chan, :]
                high = lax.reduce_precision(part, 8, 7)
                low = (part - high).astype(BF16)
                taps_in = x3[:, :frame_dev]
                products = dot(high.astype(BF16), taps_in, ((1,), (1,))) + dot(low, taps_in, ((1,), (1,)))
                for k in range(4):
                    table = table + pltpu.roll(products[k * chan : (k + 1) * chan], 128 - (m + k), 1)
    tap = iota((16, 128), 0)
    lane = iota((16, 128), 1)
    i = (tap * 11) >> 5
    select = ((lane == BAND * (tap - 3 * i) + i) & (tap < 9)) | ((lane == 3 * BAND) & (tap == 9))
    rows10 = dot(select.astype(F32), table, ((1,), (1,)), EXACT)
    share = block - 2
    mine = jnp.concatenate([summed(1 + k) for k in range(share)], axis=0)
    single = to_column(summed(block - 1), share)
    factor_l = params[2:3] * stats_two[chan : chan + 1, :chan]
    mine = mine[:, :chan] - (bias_sum * single + gain_sum * mine[:, chan:]) / total
    mine = factor_l * mine
    lower = -(-share // 2)
    mine = jnp.concatenate([mine] + [jnp.zeros((2 * lower - share, chan), F32)] * (share % 2), axis=0)
    mine = jnp.concatenate([mine[:lower], mine[lower:]], axis=1)
    if lower < 9:
        mine = jnp.concatenate([mine, jnp.zeros((9 - lower, 128), F32)], axis=0)
    sums = jnp.concatenate([rows10[0:5], rows10[5:10]], axis=1)
    block = jnp.concatenate([sums, mine], axis=0)
    for d in range(devices):
        payload[14 * d : 14 * (d + 1), :] = block


def transposed(low, w1, x3, stats, masks, ws_hbm, first, normed, ws, pre_one, sem):
    load = pltpu.make_async_copy(ws_hbm, ws, sem)
    load.start()
    chan = low.shape[0] // (MEL_ROWS + 2)
    wide = low.shape[1]
    pre_one[...] = dot(w1[2 * chan : (MEL_ROWS + 4) * chan], x3[...])
    mean = jnp.broadcast_to(stats[0:chan, 0:1], (chan, wide))
    inv = jnp.broadcast_to(stats[0:chan, 1:2], (chan, wide))
    for q in range(MEL_ROWS + 2):
        at = slice(q * chan, (q + 1) * chan)
        mask = masks[0:1] * row_valid(q - 1, MEL_ROWS)
        normed[at, :] = ((pre_one[at, :] - mean) * inv * mask).astype(BF16)
    load.wait()
    first[...] = dot(ws[...], low[...])


def finish(recv, features, stats, k1t, first, normed, ws, params, masks,
           spec_hbm, kernel_one_hbm, kernel_two_hbm, gain_hbm, bias_hbm,
           table, spec_grad, kernel_one, kernel_two, gain_out, bias_out, sems):
    chan = params.shape[1]
    rows = MEL_ROWS
    wide = normed.shape[1]
    frame_dev = wide - RIM
    usable, behind, ahead = (masks[n : n + 1] for n in range(3))
    total = masks[3:4, 0:1]
    gain = params[0:1]
    count = recv.shape[0] // 14
    share = -(-9 * chan // count)
    lower = -(-share // 2)
    left = [recv[pl.ds(5 + p, count, stride=14), :] for p in range(lower)]
    whole = jnp.concatenate([v[:, :chan] for v in left] + [v[:, chan:] for v in left], axis=0)
    for t in range(9):
        kernel_two[t] = whole[t * chan : (t + 1) * chan].T
    stores = [pltpu.make_async_copy(kernel_two, kernel_two_hbm, sems.at[3])]
    stores[0].start()
    sums = recv[0:5, :]
    for d in range(1, count):
        sums = sums + recv[14 * d : 14 * d + 5, :]
    ten = jnp.concatenate([sums[:, :chan], sums[:, chan:]], axis=0)
    bias_sum = ten[9:10]
    mean_l, inv_l = stats[chan : chan + 1, :chan], stats[chan + 8 : chan + 9, :chan]
    ten = ten - features[1:2, 0:1] * bias_sum
    k = k1t[0:9]
    gain_sum = inv_l * (jnp.sum(k * ten[0:9], axis=0, keepdims=True) - mean_l * bias_sum)
    gain_out[...] = gain_sum
    bias_out[...] = bias_sum
    for n, (source, target) in enumerate(((gain_out, gain_hbm), (bias_out, bias_hbm))):
        stores.append(pltpu.make_async_copy(source, target, sems.at[n]))
        stores[-1].start()
    factor_l = gain * inv_l
    scale = factor_l * gain_sum / total
    scale = jnp.concatenate([scale, scale], axis=1)
    scale = jnp.concatenate([scale] * ((rows + 2) // 2), axis=1)
    taps = first[...] - dot((ws[...].astype(F32) * scale).astype(BF16), normed[...])
    for part in range(wide // 128):
        table[part] = taps[:, 128 * part : 128 * (part + 1)]
    moved = [
        jnp.concatenate([table[part, pl.ds(b, rows, stride=8), :] for part in range(wide // 128)], axis=1)
        for b in range(3)
    ]
    constant = jnp.sum(k * (factor_l * bias_sum / total), axis=1, keepdims=True)
    for a in range(3):
        row = iota((rows, 1), 0) + (a - 1) + lax.axis_index("mel") * rows
        valid = ((row >= 0) & (row < lax.axis_size("mel") * rows)).astype(F32) * usable
        for b in range(3):
            t = 3 * (2 - a) + 2 - b
            moved[b] = moved[b] - constant[t : t + 1] * valid
    result = pltpu.roll(moved[0], 1, 1) * behind + moved[1] + pltpu.roll(moved[2], wide - 1, 1) * ahead
    spec_grad[0] = (result * usable)[:, :frame_dev]
    stores.append(pltpu.make_async_copy(spec_grad, spec_hbm, sems.at[2]))
    stores[-1].start()
    row = features[0:1, :]
    lane = iota((1, 128), 1)
    gram = jnp.concatenate(
        [jnp.where(lane < 9, pltpu.roll(row, 128 - 9 * t, 1) if t else row, 0.0) for t in range(9)]
        + [jnp.zeros((7, 128), F32)],
        axis=0,
    )
    single = to_column(row, 16, 81)[0:9]
    k_rows = jnp.concatenate([k1t[...], jnp.zeros((112, chan), F32)], axis=0)
    normed_taps = inv_l * (dot(gram, k_rows, precision=EXACT)[0:9] - single * mean_l)
    grad_taps = factor_l * (ten[0:9] - (bias_sum * single + gain_sum * normed_taps) / total)
    for i in range(3):
        kernel_one[i] = grad_taps[3 * i : 3 * i + 3]
    stores.append(pltpu.make_async_copy(kernel_one, kernel_one_hbm, sems.at[4]))
    stores[-1].start()
    for store in stores:
        store.wait()


def run(kernel, outs, scratch, *args, hbm=0, apart=(), flops=10**8, size=4 * 10**6):
    vmem = pl.BlockSpec(memory_space=pltpu.VMEM)
    specs = []
    args = list(args)
    for n, a in enumerate(args):
        if hbm and n >= len(args) - hbm:
            specs.append(pl.BlockSpec(memory_space=pltpu.HBM))
            args[n] = pltpu.with_memory_space_constraint(a, pltpu.HBM)
        else:
            specs.append(vmem)
            args[n] = pltpu.with_memory_space_constraint(a, pltpu.VMEM)
    return pl.pallas_call(
        kernel,
        out_shape=outs,
        in_specs=specs,
        out_specs=[pl.BlockSpec(memory_space=pltpu.HBM) if n in apart else vmem for n in range(len(outs))],
        scratch_shapes=scratch,
        compiler_params=pltpu.CompilerParams(vmem_limit_bytes=30 * 2**20),
        cost_estimate=pl.CostEstimate(flops=flops, bytes_accessed=size, transcendentals=0),
    )(*args)


def shape(dims, dtype=F32):
    return jax.ShapeDtypeStruct(dims, dtype)


def kept(dims, dtype=F32):
    return pltpu.VMEM(dims, dtype)


def far(dims, dtype=F32):
    return pltpu.HBM(dims, dtype)


def exchange(blocks, axes=AXES):
    return lax.all_to_all(blocks, axes, 0, 0, tiled=True)


def exchange_rows(rows, axes=AXES):
    return exchange(rows[:, None, :], axes)[:, 0, :]


def shards(spectrum, clip_bounds, kernel_one, gain_one, bias_one, kernel_two, gain_two, bias_two, pooled_grad):
    _, rows, frame_dev = spectrum.shape
    chan = kernel_two.shape[0]
    n_mel, n_tm = lax.axis_size("mel"), lax.axis_size("tm")
    devices = n_mel * n_tm
    half = frame_dev // 2
    wide = frame_dev + RIM
    mels = n_mel * rows

    packed, own = run(
        pack_mel,
        [kept((n_mel, 2 * rows + chan, half), BF16), kept(pooled_grad.shape, BF16)],
        [
            pltpu.VMEM(spectrum.shape, BF16),
            pltpu.SemaphoreType.DMA((2,)),
        ],
        spectrum,
        pooled_grad,
        hbm=2,
    )
    recv_mel = exchange(packed, "mel")
    ext = rows + 6
    span = 4 * 3 * chan
    wf, wb, w1, ws, pairs, singles, k1t, params, masks, edge_masks, twice, own_rows = run(
        weights,
        [
            kept((2 * chan, span), BF16),
            kept((2 * chan, span), BF16),
            kept((ext * chan, 128), BF16),
            far((rows * 8, (rows + 2) * chan), BF16),
            kept((chan, 128)),
            kept((chan, 128)),
            kept((16, chan)),
            kept((8, chan)),
            kept((8, wide)),
            kept((n_tm * 8, 128)),
            kept((128, 128)),
            kept((chan * rows // 2, half), BF16),
        ],
        [
            pltpu.VMEM((9, chan, chan), BF16),
            pltpu.VMEM((3, 3, chan), BF16),
            pltpu.VMEM((4, 1, chan), F32),
            pltpu.SMEM(clip_bounds.shape, jnp.int32),
            pltpu.VMEM((rows * 8, (rows + 2) * chan), BF16),
            pltpu.VMEM((chan * rows // 2, half), F32),
            pltpu.SemaphoreType.DMA((8,)),
        ],
        own,
        clip_bounds,
        jnp.transpose(kernel_two, (2, 3, 0, 1)).reshape(9, chan, chan),
        jnp.transpose(kernel_one, (1, 2, 0)),
        gain_one[None],
        bias_one[None],
        gain_two[None],
        bias_two[None],
        hbm=7,
        apart=(3,),
    )
    (packed,) = run(
        pack_tm,
        [kept((n_tm, 16, 128), BF16)],
        [pltpu.VMEM((n_tm * 16, 128), F32)],
        recv_mel,
        own_rows,
        masks,
    )
    recv_tm = exchange(packed, "tm")
    pre_two, payload, act, x3, stats_one, features = run(
        forward_one,
        [
            kept(((rows + 4) * chan, wide)),
            kept((devices, 128)),
            kept((ext * 3 * chan, wide), BF16),
            kept((128, wide), BF16),
            kept((2 * chan + 16, 128)),
            kept((8, 128)),
        ],
        [pltpu.VMEM((ext * chan, wide), F32), pltpu.VMEM((mels + 8, wide), F32)],
        recv_mel,
        recv_tm,
        pairs,
        singles,
        twice,
        w1,
        wf,
        params,
        masks,
        edge_masks,
    )
    recv = exchange_rows(payload)
    grad, payload, row_pairs, stats_two = run(
        backward_scaled,
        [
            kept(((rows + 4) * chan, wide)),
            kept((devices * sum_rows(devices, 9 * chan), 128)),
            far((rows // 2 * chan, frame_dev)),
            kept((chan + 8, 128)),
        ],
        [
            pltpu.VMEM(((rows // 2 + 2) * chan, RIM), F32),
            pltpu.VMEM((rows // 2 * chan, frame_dev), F32),
            pltpu.VMEM((3 * chan + 16, rows * frame_dev), BF16),
            pltpu.SemaphoreType.DMA((rows // 4,)),
        ],
        recv,
        pre_two,
        act,
        recv_mel,
        recv_tm,
        own_rows,
        params,
        masks,
        apart=(2,),
    )
    recv = exchange_rows(payload)
    low, payload, gain_two_grad, bias_two_grad = run(
        backward,
        [
            kept(((rows + 2) * chan, wide), BF16),
            kept((devices * 14, 128)),
            shape((1, chan)),
            shape((1, chan)),
        ],
        [
            pltpu.VMEM(((rows + 4) * 3 * chan, wide), BF16),
            pltpu.VMEM(((rows + 2) * chan, wide), F32),
            pltpu.VMEM((rows * chan, frame_dev), F32),
        ],
        recv,
        pre_two,
        grad,
        stats_two,
        w1,
        x3,
        stats_one,
        params,
        masks,
        wb,
    )
    recv = exchange_rows(payload)
    (pooled,) = run(
        pool,
        [shape((1, chan, rows // 2, half), BF16)],
        [
            pltpu.VMEM((rows // 2 * chan, 128), F32),
            pltpu.VMEM((rows // 2 * chan, frame_dev), F32),
            pltpu.SemaphoreType.DMA,
        ],
        payload,
        row_pairs,
        hbm=1,
    )
    first, normed, ws = run(
        transposed,
        [
            kept((rows * 8, wide)),
            kept(((rows + 2) * chan, wide), BF16),
            kept((rows * 8, (rows + 2) * chan), BF16),
        ],
        [pltpu.VMEM(((rows + 2) * chan, wide), F32), pltpu.SemaphoreType.DMA],
        low,
        w1,
        x3,
        stats_one,
        masks,
        ws,
        hbm=1,
    )
    spec_grad, kernel_one_grad, kernel_two_grad, gain_one_grad, bias_one_grad = run(
        finish,
        [
            shape((1, rows, frame_dev)),
            shape((3, 3, chan)),
            shape((9, chan, chan)),
            shape((1, chan)),
            shape((1, chan)),
        ],
        [
            pltpu.VMEM((3, rows * 8, 128), F32),
            pltpu.VMEM((1, rows, frame_dev), F32),
            pltpu.VMEM((3, 3, chan), F32),
            pltpu.VMEM((9, chan, chan), F32),
            pltpu.VMEM((1, chan), F32),
            pltpu.VMEM((1, chan), F32),
            pltpu.SemaphoreType.DMA((5,)),
        ],
        recv,
        features,
        stats_one,
        k1t,
        first,
        normed,
        ws,
        params,
        masks,
        apart=range(5),
    )
    kernel_two_grad = jnp.transpose(kernel_two_grad.reshape(3, 3, chan, chan), (2, 3, 0, 1))
    return (
        pooled,
        spec_grad,
        jnp.transpose(kernel_one_grad, (2, 0, 1)),
        gain_one_grad[0],
        bias_one_grad[0],
        kernel_two_grad,
        gain_two_grad[0],
        bias_two_grad[0],
    )


def solution(mesh):
    return jax.shard_map(
        shards,
        mesh=mesh,
        in_specs=(
            P(None, "mel", "tm"),
            P(),
            P(),
            P(),
            P(),
            P(),
            P(),
            P(),
            P(None, None, "mel", "tm"),
        ),
        out_specs=(P(None, None, "mel", "tm"), P(None, "mel", "tm"), P(), P(), P(), P(), P(), P()),
        check_vma=False,
    )
```

```python
import functools

import jax
import jax.numpy as jnp
from jax import lax
from jax.experimental import pallas as pl
from jax.experimental.pallas import tpu as pltpu
from jax.sharding import PartitionSpec as P

F32 = jnp.float32
BF16 = jnp.bfloat16
AXES = ("mel", "tm")
EXACT = lax.Precision.HIGHEST
RIM = 128
BAND = 24
MEL_ROWS = 16
FIRST = 24
SUMS, EDGES, COLUMNS = 16, 19, 23
SIDE = 96
SECOND = 8


def iota(shape, dim):
    return lax.broadcasted_iota(jnp.int32, shape, dim)


def dot(a, b, over=((1,), (0,)), precision=None):
    return lax.dot_general(a, b, (over, ((), ())), precision=precision, preferred_element_type=F32)


def to_column(lanes, count, start=0):
    shape = (count, lanes.shape[1])
    return jnp.sum(jnp.where(iota(shape, 1) == iota(shape, 0) + start, lanes, 0.0), axis=1, keepdims=True)


def to_lanes(column, start=0, width=128):
    shape = (column.shape[0], width)
    return jnp.sum(jnp.where(iota(shape, 1) == iota(shape, 0) + start, column, 0.0), axis=0, keepdims=True)


def halves(v):
    total = v[:, :128]
    for n in range(128, v.shape[1], 128):
        total = total + v[:, n : n + 128]
    return total


def frame_masks(bounds, frames):
    last = bounds.shape[1] - 1

    def living(f):
        return (f >= 0) & (f < bounds[0, last])

    def paired(f):
        both = living(f) & living(f + 1)
        for k in range(1, last):
            both = both & (f + 1 != bounds[0, k])
        return both

    return tuple(m.astype(F32) for m in (living(frames), paired(frames - 1), paired(frames)))


def row_valid(row, rows):
    mel = lax.axis_index("mel") * rows + row
    return ((mel >= 0) & (mel < lax.axis_size("mel") * rows)).astype(F32)


def start_all(*pairs, sems):
    copies = [pltpu.make_async_copy(src, dst, sems.at[n]) for n, (src, dst) in enumerate(pairs)]
    for copy in copies:
        copy.start()
    return copies


def wait_all(copies):
    for copy in copies:
        copy.wait()


def shifted_frames(value, behind, ahead):
    wide = value.shape[1]
    return pltpu.roll(value, 1, 1) * behind, pltpu.roll(value, wide - 1, 1) * ahead


def three_parts(v):
    high = lax.reduce_precision(v, 8, 7)
    mid = lax.reduce_precision(v - high, 8, 7)
    return high, mid, v - high - mid


def share_of(devices, chan):
    return -(-chan // devices)


def pack(spec_hbm, grad_hbm, bounds_hbm, out, own, spec, masks, bounds, edges, rows_out, sems):
    copies = start_all((bounds_hbm, bounds), (spec_hbm, spec), (grad_hbm, own), sems=sems)
    copies[0].wait()
    wide = masks.shape[1]
    frame_dev = wide - RIM
    devices = out.shape[0]
    rows = MEL_ROWS
    lane = iota((1, wide), 1)
    frames = lax.axis_index("tm") * frame_dev + jnp.where(lane < frame_dev + RIM // 2, lane, lane - wide)
    last = bounds.shape[1] - 1
    pixels = (bounds[0, last] * (lax.axis_size("mel") * rows)).astype(F32)
    found = frame_masks(bounds, frames)
    masks[...] = jnp.concatenate(
        list(found) + [jnp.full((1, wide), 1.0) * pixels, jnp.zeros((4, wide), F32)], axis=0
    )
    usable, behind, ahead = (m[:, :frame_dev] for m in found)
    copies[1].wait()
    x = spec[0].astype(F32) * usable
    lane = iota((1, frame_dev), 1)
    row = iota((rows, 1), 0)
    inner = jnp.where((lane > 0) & (lane < frame_dev - 1), usable, 0.0)
    number = (rows - 2) * jnp.sum(inner, axis=1, keepdims=True)
    inner = inner * ((row > 0) & (row < rows - 1)).astype(F32)
    centre = jnp.sum(jnp.sum(x, axis=0, keepdims=True), axis=1, keepdims=True)
    centre = centre / (rows * jnp.maximum(jnp.sum(usable, axis=1, keepdims=True), 1.0))
    centre = lax.reduce_precision(centre, 8, 7)
    shifted = [pltpu.roll(x, 1, 1) * behind, x, pltpu.roll(x, frame_dev - 1, 1) * ahead]
    features = feature_rows(
        [pltpu.roll(shifted[j], (1 - i) % rows, 0) if i != 1 else shifted[j] for i in range(3) for j in range(3)],
        inner,
        centre,
    )
    lane = iota((1, 128), 1)
    features = jnp.where(lane == 90, centre, jnp.where(lane == 91, number, features))
    pick = iota((8, frame_dev), 0)
    column = jnp.where(pick < 4, pick, frame_dev - 8 + pick)
    strip = dot((iota((8, frame_dev), 1) == column).astype(BF16), x.astype(BF16), ((1,), (1,)))
    lane = iota((8, 128), 1)
    repeat = (iota((rows, 128), 1) % rows == iota((rows, 128), 0)).astype(BF16)
    strip = jnp.where(lane // rows == iota((8, 128), 0), dot(strip.astype(BF16), repeat), 0.0)
    strip = jnp.sum(strip, axis=0, keepdims=True)

    def put(n, value):
        rows_out[pl.ds(n, devices, stride=FIRST), :] = jnp.broadcast_to(value, (devices, 128))

    near = jnp.concatenate([x[0:4], x[rows - 4 :]], axis=0)
    for n in range(8):
        put(n, near[n : n + 1, :128])
        put(8 + n, near[n : n + 1, 128:])
    put(COLUMNS, strip)
    copies[2].wait()
    _, chan, many, half = own.shape
    share = share_of(devices, chan)
    holders = chan // share
    g = own[0].astype(F32)
    edges[0:chan] = g[:, 0, :]
    edges[chan:] = g[:, many - 1, :]

    def spread_out(v):
        if holders < devices:
            v = jnp.concatenate([v, jnp.zeros((devices - holders, 128), F32)], axis=0)
        return v

    for n in range(share):
        put(EDGES + n, spread_out(edges[pl.ds(n, holders, stride=share), :]))
        put(EDGES + share + n, spread_out(edges[pl.ds(chan + n, holders, stride=share), :]))
    for n in range(2 * share, COLUMNS - EDGES):
        put(EDGES + n, jnp.zeros((1, 128), F32))
    end = iota((8, half), 0)
    at = iota((8, half), 1)
    ends = ((end == 0) & (at == 0)) | ((end == 1) & (at == half - 1))
    columns = dot(ends.astype(BF16), g.reshape(chan * many, half).astype(BF16), ((1,), (1,)))
    per = share * many
    group = 128 // per
    source = iota((128, 128), 0)
    move = (iota((128, 128), 1) == SIDE + source % per).astype(BF16)
    lane = iota((group, 128), 1)
    mine = lane // per == iota((group, 128), 0)
    parts = three_parts(features)
    for n in range(2):
        side = jnp.concatenate(
            [jnp.where(mine, columns[n : n + 1, 128 * q : 128 * (q + 1)], 0.0) for q in range(chan * many // 128)],
            axis=0,
        )
        put(SUMS + n, spread_out(dot(side.astype(BF16), move)) + parts[n])
    put(SUMS + 2, parts[2])
    out[...] = rows_out[...].reshape(out.shape).astype(BF16)


def weights(own, bounds_hbm, k2_hbm, k1_hbm, gain_one_hbm, bias_one_hbm, gain_two_hbm, bias_two_hbm,
            wf, wb, w1, ws_hbm, pairs, singles, k1t, params, all_masks, edge_masks, twice, own_rows,
            k2, k1, vectors, bounds, ws, temp, sems):
    loads = start_all(
        (bounds_hbm, bounds),
        (k2_hbm, k2),
        (k1_hbm, k1),
        (gain_one_hbm, vectors.at[0]),
        (bias_one_hbm, vectors.at[1]),
        (gain_two_hbm, vectors.at[2]),
        (bias_two_hbm, vectors.at[3]),
        sems=sems,
    )
    _, many, count, half = own.shape
    temp[...] = own[0].astype(F32).reshape(many * count, half)
    for r in range(count):
        own_rows[r * many : (r + 1) * many] = temp[pl.ds(r, many, stride=count), :].astype(BF16)
    wait_all(loads)
    chan = k2.shape[1]
    span = wf.shape[1]
    taps = [k2[t].astype(F32) for t in range(9)]
    rest = jnp.zeros((chan, span - 9 * chan), F32)
    forward = jnp.concatenate(taps + [rest], axis=1)
    backward = jnp.concatenate([taps[8 - t].T for t in range(9)] + [rest], axis=1)
    for r in range(wb.shape[0] // chan):
        at = slice(r * chan, (r + 1) * chan)
        wb[at] = (pltpu.roll(backward, 3 * chan * r, 1) if r else backward).astype(BF16)
    full = jnp.concatenate([k1[n].astype(F32) for n in range(3)] + [jnp.zeros((7, chan), F32)], axis=0)
    low = [
        jnp.concatenate([full[3 * (2 - a) + 2 - b : 3 * (2 - a) + 3 - b] for a in range(3)], axis=1)
        for b in range(3)
    ]
    base = jnp.concatenate(low + [jnp.zeros((5, 3 * chan), F32)], axis=0)
    base = jnp.concatenate([base, jnp.zeros((8, ws.shape[1] - 3 * chan), F32)], axis=1)
    for m in range(ws.shape[0] // 8):
        ws[8 * m : 8 * m + 8] = (pltpu.roll(base, chan * m, 1) if m else base).astype(BF16)
    store_ws = pltpu.make_async_copy(ws, ws_hbm, sems.at[7])
    store_ws.start()
    frames = all_masks.shape[1]
    frame_dev = frames // lax.axis_size("tm")
    all_masks[...] = jnp.concatenate(
        list(frame_masks(bounds, iota((1, frames), 1))) + [jnp.zeros((5, frames), F32)], axis=0
    )
    q = iota(edge_masks.shape, 0)
    lane = iota(edge_masks.shape, 1)
    k = q % 8
    frames = (q // 8) * frame_dev + jnp.where(k < 4, k, k + frame_dev - 8)
    living, behind, ahead = frame_masks(bounds, frames)
    living = jnp.where((k == 0) | (k == 7), living, 0.0)
    edge_masks[...] = jnp.where(lane == 0, living, jnp.where(lane == 1, behind, jnp.where(lane == 2, ahead, 0.0)))
    params[...] = jnp.concatenate(
        [vectors[n] for n in range(4)] + [jnp.zeros((4, chan), F32)], axis=0
    )
    tap = iota((16, 128), 0)
    lane = iota((16, 128), 1)
    i = (tap * 11) >> 5
    ninth = (lane * 57) >> 9
    to_band = (lane == BAND * (tap - 3 * i) + i) & (tap < 9)
    to_left = (ninth == tap) & (tap < 9)
    to_right = (lane - 9 * ninth == tap) & (lane < 81)
    to_single = (lane == 81 + tap) & (tap < 9)
    source = iota((128, 128), 0) - 81
    lane = iota((128, 128), 1)
    ninth = (lane * 57) >> 9
    inside = (source >= 0) & (source < 9) & (lane < 81)
    twice[...] = jnp.where(inside, (source == ninth).astype(F32) + (source == lane - 9 * ninth).astype(F32), 0.0)
    for r in range(wf.shape[0] // chan):
        at = slice(r * chan, (r + 1) * chan)
        wf[at] = (pltpu.roll(forward, 3 * chan * r, 1) if r else forward).astype(BF16)
    k1t[...] = full
    k = full.astype(BF16)
    lanes = [dot(k, select.astype(BF16), ((0,), (0,))) for select in (to_band, to_left, to_right, to_single)]
    pairs[...] = lanes[1] * lanes[2]
    singles[...] = lanes[3]
    for m in range(w1.shape[0] // chan):
        w1[m * chan : (m + 1) * chan] = (pltpu.roll(lanes[0], m, 1) if m else lanes[0]).astype(BF16)
    store_ws.wait()


def feature_rows(taps, weight, centre):
    z = [tap - centre for tap in taps]

    def folded(v):
        return jnp.sum(halves(v), axis=0, keepdims=True)

    rows = [None] * 96
    for s in range(9):
        left = z[s] * weight
        rows[81 + s] = folded(left)
        for t in range(s, 9):
            rows[9 * s + t] = rows[9 * t + s] = folded(left * z[t])
    zero = jnp.zeros((1, 128), F32)
    stack = jnp.concatenate([zero if r is None else r for r in rows], axis=0)
    return to_lanes(jnp.sum(stack, axis=1, keepdims=True))


def moved_rows(v, step):
    if step == 0:
        return v
    count = v.shape[0]
    if abs(step) >= count:
        return jnp.zeros_like(v)
    zero = jnp.zeros((abs(step), v.shape[1]), v.dtype)
    if step > 0:
        return jnp.concatenate([zero, v[: count - step]], axis=0)
    return jnp.concatenate([v[-step:], zero], axis=0)


def silu_halves(h):
    t = jnp.tanh(h)
    one = 1.0 + t
    return h * one, one * (1.0 + h * (1.0 - t))


def forward_one(recv, spec, pairs, singles, twice, w1, wf, params, masks, all_masks, edge_masks,
                pre_two, payload, act, x3, stats, features_out, pre_one, got, strips, halo, rows_out):
    devices = recv.shape[0]
    n_mel, count = lax.axis_size("mel"), lax.axis_size("tm")
    rows = MEL_ROWS
    mels = n_mel * rows
    wide = masks.shape[1]
    frame_dev = wide - RIM
    chan = params.shape[1]
    me_m, me_t = lax.axis_index("mel"), lax.axis_index("tm")
    usable, behind, ahead = (masks[n : n + 1] for n in range(3))
    total = masks[3:4, 0:1]
    got[...] = recv[...].astype(F32).reshape(devices * FIRST, 128)

    def every(n):
        return got[pl.ds(n, devices, stride=FIRST), :]

    lane = iota((count, 128), 1)
    bands = [got[pl.ds(FIRST * k * count + COLUMNS, count, stride=FIRST), :] for k in range(n_mel)]
    for c in range(8):
        column = jnp.zeros((count, 128), F32)
        for k, band in enumerate(bands):
            part = jnp.where(lane // rows == c, band, 0.0)
            column = column + (pltpu.roll(part, rows * (k - c) % 128, 1) if k != c else part)
        strips[pl.ds(c, count, stride=8), :] = column
    at = pl.multiple_of(FIRST * (jnp.maximum(me_m - 1, 0) * count + me_t), 8)
    above = got[pl.ds(at, 16), :] * (me_m > 0).astype(F32)
    at = pl.multiple_of(FIRST * (jnp.minimum(me_m + 1, n_mel - 1) * count + me_t), 8)
    below = got[pl.ds(at, 16), :] * (me_m < n_mel - 1).astype(F32)
    above = jnp.concatenate([above[4:8], above[12:16]], axis=1)
    below = jnp.concatenate([below[0:4], below[8:12]], axis=1)
    own = spec[0].astype(F32) * usable[:, :frame_dev]
    at = pl.multiple_of(8 * jnp.minimum(me_t + 1, count - 1), 8)
    after = strips[pl.ds(at, 8), :][:, :mels] * (me_t + 1 < count).astype(F32)
    at = pl.multiple_of(8 * jnp.maximum(me_t - 1, 0), 8)
    before = strips[pl.ds(at, 8), :][:, :mels] * (me_t > 0).astype(F32)
    sides = jnp.concatenate([after[0:4], before[4:8], jnp.zeros((8, mels), F32)], axis=0).astype(BF16)
    side = iota((16, RIM), 0)
    place = iota((16, RIM), 1) == jnp.where(side < 4, side, jnp.where(side < 8, side + RIM - 8, -1))
    halo[0:8] = jnp.zeros((8, RIM), F32)
    halo[mels : mels + 8] = jnp.zeros((8, RIM), F32)
    halo[4 : mels + 4] = dot(sides, place.astype(BF16), ((0,), (0,)))
    rim = halo[pl.ds(pl.multiple_of(me_m * rows, 8), BAND), :]
    near = jnp.concatenate([jnp.concatenate([above, own, below], axis=0), rim], axis=1)
    x3[...] = jnp.concatenate(
        [
            pltpu.roll(near, 1, 1) * behind,
            near,
            pltpu.roll(near, wide - 1, 1) * ahead,
            jnp.broadcast_to(usable, (BAND, wide)),
            jnp.zeros((128 - 4 * BAND, wide), F32),
        ],
        axis=0,
    ).astype(BF16)
    pre_one[...] = dot(w1[...], x3[...])
    lane = iota((1, 128), 1)
    parts = jnp.where(lane < 92, every(SUMS) + every(SUMS + 1) + every(SUMS + 2), 0.0)
    centres, numbers = parts[:, 90:91], parts[:, 91:92]
    centre = jnp.sum(centres * numbers, axis=0, keepdims=True)
    centre = centre / jnp.maximum(jnp.sum(numbers, axis=0, keepdims=True), 1.0)
    delta = centres - centre
    features = jnp.sum(parts + delta * numbers * jnp.where(lane < 81, delta, 1.0), axis=0, keepdims=True)
    moved = jnp.sum(delta * parts, axis=0, keepdims=True)
    moved = dot(jnp.broadcast_to(moved, (8, 128)), twice[...], precision=EXACT)[0:1]
    features = features + moved
    tiles = []
    for k in range(n_mel):
        lanes = []
        for d in range(count):
            at = FIRST * (k * count + d)
            lanes += [got[at : at + 8, :], got[at + 8 : at + 16, :]]
        tiles.append(jnp.concatenate(lanes, axis=1))
    zero = jnp.zeros((1, tiles[0].shape[1]), F32)
    before_row, this_row, next_row = [], [], []
    for k, tile in enumerate(tiles):
        before_row += [tiles[k - 1][7:8] if k else zero, tile[6:7]]
        this_row += [tile[0:1], tile[7:8]]
        next_row += [tile[1:2], tiles[k + 1][0:1] if k + 1 < n_mel else zero]
    f_usable, f_behind, f_ahead = (all_masks[n : n + 1] for n in range(3))
    taps = []
    for group in (before_row, this_row, next_row):
        v = jnp.concatenate(group, axis=0)
        taps += [pltpu.roll(v, 1, 1) * f_behind, v, pltpu.roll(v, v.shape[1] - 1, 1) * f_ahead]
    features = features + feature_rows(taps, f_usable, centre)
    edge = strips[...]
    q_usable, q_behind, q_ahead = (edge_masks[:, n : n + 1] for n in range(3))
    lane = iota((count * 8, 128), 1)
    inside = (lane < mels) & (lane % rows != 0) & (lane % rows != rows - 1)
    shifted = [
        pltpu.roll(edge, 1, 0) * q_behind,
        edge,
        pltpu.roll(edge, count * 8 - 1, 0) * q_ahead,
    ]
    taps = [pltpu.roll(v, (1 - i) % 128, 1) if i != 1 else v for i in range(3) for v in shifted]
    features = features + feature_rows(taps, jnp.where(inside, q_usable, 0.0), centre)
    features = jnp.where(iota((1, 128), 1) < 90, features, 0.0)
    features_out[...] = jnp.concatenate(
        [features, jnp.broadcast_to(centre, (1, 128)), jnp.zeros((6, 128), F32)], axis=0
    )
    near_mean = jnp.sum(singles[...] * features, axis=1, keepdims=True) / total
    square = jnp.sum(pairs[...] * features, axis=1, keepdims=True) / total
    inv = lax.rsqrt(square - near_mean * near_mean + 1e-05)
    mean = near_mean + centre * jnp.sum(singles[...], axis=1, keepdims=True)
    lane = iota((chan, 128), 1)
    stats[0:chan] = jnp.where(lane == 0, mean, jnp.where(lane == 1, inv, 0.0))
    stats[chan : chan + 8] = jnp.broadcast_to(to_lanes(near_mean), (8, 128))
    stats[chan + 8 : chan + 16] = jnp.broadcast_to(to_lanes(inv), (8, 128))
    scale = 0.5 * to_column(params[0:1], chan) * inv
    shift = 0.5 * to_column(params[1:2], chan) - mean * scale
    stats[chan + 16 :] = jnp.where(lane == 0, scale, jnp.where(lane == 1, shift, 0.0))
    scale = jnp.broadcast_to(scale, (chan, wide))
    shift = jnp.broadcast_to(shift, (chan, wide))
    ext = w1.shape[0] // chan
    block, taps = wf.shape
    first = jnp.zeros((chan, 128), F32)
    second = jnp.zeros((chan, 128), F32)
    own_mask = usable[:, :frame_dev]
    low_masks = [m.astype(BF16) for m in (usable, behind, ahead)]
    for r in range(ext):
        value, _ = silu_halves(pre_one[r * chan : (r + 1) * chan, :] * scale + shift)
        if not 0 <= r - 3 < rows:
            value = value * row_valid(r - 3, rows)
        base = r * 3 * chan
        low = value.astype(BF16) * low_masks[0]
        act[base : base + chan, :], act[base + 2 * chan : base + 3 * chan, :] = shifted_frames(low, *low_masks[1:])
        act[base + chan : base + 2 * chan, :] = low
        if r < 3 or r % 2 == 0:
            continue
        g = (r - 3) // 2
        result = dot(wf[...], act[g * 3 * block : g * 3 * block + taps, :])
        pre_two[g * block : (g + 1) * block] = result
        for q in range(2):
            if 2 <= 2 * g + q < rows + 2:
                p = result[q * chan : (q + 1) * chan, :frame_dev]
                masked = p * own_mask
                first = first + halves(masked)
                second = second + halves(masked * p)
    share = share_of(devices, chan)

    def put(n, value):
        rows_out[pl.ds(n, devices, stride=SECOND), :] = jnp.broadcast_to(value, (devices, 128))

    for n in range(share):
        put(3 + n, moved_rows(every(EDGES + share + n), count))
        put(3 + share + n, moved_rows(every(EDGES + n), -count))
    for n in range(3 + 2 * share, SECOND - 1):
        put(n, jnp.zeros((1, 128), F32))
    lane = iota((devices, 128), 1)
    tm = iota((devices, 128), 0) % count
    lefts = jnp.where(lane >= SIDE, every(SUMS), 0.0)
    rights = jnp.where(lane >= SIDE, every(SUMS + 1), 0.0)
    beside = jnp.zeros((devices, 128), F32)
    for n, step in enumerate((0, count, -count)):
        one = jnp.where(tm > 0, moved_rows(rights, step + 1), 0.0)
        two = jnp.where(tm < count - 1, moved_rows(lefts, step - 1), 0.0)
        beside = beside + pltpu.roll(one, (32 * n - SIDE) % 128, 1) + pltpu.roll(two, (32 * n + 16 - SIDE) % 128, 1)
    put(SECOND - 1, beside)
    first = jnp.sum(first, axis=1, keepdims=True)
    second = jnp.sum(second, axis=1, keepdims=True)
    for n, part in enumerate(three_parts(to_lanes(first) + to_lanes(second, chan))):
        put(n, part)
    payload[...] = rows_out[...].reshape(payload.shape).astype(BF16)


def sum_rows(devices, taps):
    return -(-taps // devices) + 2


def backward_scaled(recv, pre_two, act, own_rows, params, masks,
                    grad, payload, pairs_hbm, stats, sides, pairs, right, got, beyond, sems):
    devices = recv.shape[0]
    got[...] = recv[...].astype(F32).reshape(devices * SECOND, 128)
    chan = params.shape[1]
    half = own_rows.shape[1]
    lane = iota((half, 2 * half), 1)
    spread = jnp.where(lane >> 1 == iota((half, 2 * half), 0), 0.25, 0.0).astype(BF16)
    rows = MEL_ROWS
    wide = pre_two.shape[1]
    frame_dev = wide - RIM
    usable = masks[0:1]
    share = share_of(devices, chan)
    holders = chan // share

    def every(n):
        return got[pl.ds(n, devices, stride=SECOND), :]

    beside = every(SECOND - 1)[:holders]
    lane = iota((holders, RIM), 1)
    many = rows // 2
    for n in range(share):
        beyond[pl.ds(n, holders, stride=share), :] = every(3 + n)[:holders]
        beyond[pl.ds(chan + n, holders, stride=share), :] = every(3 + share + n)[:holders]
        for r in range(many + 2):
            at = many * n + (r if r < many else 32 + many - 1 if r == many else 64)
            left, right_of = beside[:, at : at + 1], beside[:, at + 16 : at + 17]
            side = jnp.where(lane >= RIM - 2, 0.25 * left, jnp.where(lane < 2, 0.25 * right_of, 0.0))
            sides[pl.ds(r * chan + n, holders, stride=share), :] = side
    total = masks[3:4, 0:1]
    sums = jnp.sum(every(0) + every(1) + every(2), axis=0, keepdims=True)
    mean = to_column(sums, chan) / total
    inv = lax.rsqrt(to_column(sums, chan, chan) / total - mean * mean + 1e-05)
    lane = iota((chan, 128), 1)
    stats[0:chan] = jnp.where(lane == 0, mean, jnp.where(lane == 1, inv, 0.0))
    stats[chan : chan + 8] = jnp.broadcast_to(to_lanes(inv), (8, 128))
    scale = 0.5 * to_column(params[2:3], chan) * inv
    shift = jnp.broadcast_to(0.5 * to_column(params[3:4], chan) - mean * scale, (chan, wide))
    scale = jnp.broadcast_to(scale, (chan, wide))
    mean = jnp.broadcast_to(mean, (chan, frame_dev))
    inv = jnp.broadcast_to(inv, (chan, frame_dev))
    first = jnp.zeros((chan, 128), F32)
    second = jnp.zeros((chan, 128), F32)
    own_mask = usable[:, :frame_dev]
    right[3 * chan :] = jnp.ones((16, rows * frame_dev), BF16)
    table = jnp.zeros((9 * chan, 3 * chan + 16), F32)
    stores = []
    for q in list(range(2, rows + 2)) + [0, 1, rows + 2, rows + 3]:
        r = q // 2
        at = slice(q * chan, (q + 1) * chan)
        m = q - 2
        mask = 0.5 * usable if 0 <= m < rows else usable * (0.5 * row_valid(m, rows))
        if q % 2 == 0:
            if 1 <= r <= rows // 2:
                pooled, at_side = own_rows[(r - 1) * chan : r * chan], (r - 1) * chan
            elif r == 0:
                pooled, at_side = beyond[0:chan].astype(BF16), many * chan
            else:
                pooled, at_side = beyond[chan:].astype(BF16), (many + 1) * chan
            up = jnp.concatenate([dot(pooled, spread), sides[at_side : at_side + chan, :]], axis=1)
        pre = pre_two[at, :]
        value, slope = silu_halves(pre * scale + shift)
        g = up * slope * mask
        grad[at, :] = g
        if not 0 <= m < rows:
            continue
        g = g[:, :frame_dev]
        normed = (pre[:, :frame_dev] - mean) * inv
        first = first + halves(g * normed)
        second = second + halves(g)
        value = value[:, :frame_dev] * own_mask
        both = value if q % 2 == 0 else both + value
        if q % 2:
            pairs[(r - 1) * chan : r * chan, :] = both
            if r % 2 == 0:
                part = pl.ds((r - 2) * chan, 2 * chan)
                stores.append(pltpu.make_async_copy(pairs.at[part, :], pairs_hbm.at[part, :], sems.at[r // 2 - 1]))
                stores[-1].start()
        lanes = slice(m * frame_dev, (m + 1) * frame_dev)
        high = lax.reduce_precision(g, 8, 7)
        right[0:chan, lanes] = high.astype(BF16)
        right[chan : 2 * chan, lanes] = (g - high).astype(BF16)
        right[2 * chan : 3 * chan, lanes] = normed.astype(BF16)
        if m % 4 == 3:
            left = [act[(n + 2) * 3 * chan : (n + 5) * 3 * chan, :frame_dev] for n in range(m - 3, m + 1)]
            lanes = slice((m - 3) * frame_dev, (m + 1) * frame_dev)
            table = table + dot(jnp.concatenate(left, axis=1), right[:, lanes], ((1,), (1,)))
    first = jnp.sum(first, axis=1, keepdims=True)
    second = jnp.sum(second, axis=1, keepdims=True)
    totals = to_lanes(first) + to_lanes(second, chan)
    block = payload.shape[0] // devices
    payload[pl.ds(0, devices, stride=block), :] = jnp.broadcast_to(totals, (devices, 128))
    both = jnp.concatenate([table[:, :chan] + table[:, chan : 2 * chan], table[:, 2 * chan : 3 * chan]], axis=1)
    single = table[:, 3 * chan : 3 * chan + 1]
    lane = iota((devices, 128), 1)
    constants = jnp.zeros((devices, 128), F32)
    for k in range(block - 2):
        cut, ones = both[k * devices : (k + 1) * devices], single[k * devices : (k + 1) * devices]
        short = devices - cut.shape[0]
        if short:
            cut = jnp.concatenate([cut, jnp.zeros((short, 128), F32)], axis=0)
            ones = jnp.concatenate([ones, jnp.zeros((short, 1), F32)], axis=0)
        payload[pl.ds(1 + k, devices, stride=block), :] = cut
        constants = jnp.where(lane == k, ones, constants)
    payload[pl.ds(block - 1, devices, stride=block), :] = constants
    for store in stores:
        store.wait()


def pool(after, pairs_hbm, out, temp, pairs, sem):
    del after
    load = pltpu.make_async_copy(pairs_hbm, pairs, sem)
    load.start()
    chan, rows, half = out.shape[1:]
    to_mean = jnp.where(iota((2 * half, half), 0) >> 1 == iota((2 * half, half), 1), 0.25, 0.0)
    load.wait()
    pooled = dot(pairs[...], to_mean, precision=EXACT)
    for r in range(rows):
        temp[pl.ds(r, chan, stride=rows), :] = pooled[r * chan : (r + 1) * chan]
    out[0] = temp[...].reshape(chan, rows, half).astype(BF16)


def backward(recv, pre_two, grad, stats_two, w1, x3, stats, params, masks, wb,
             out, payload, gain_out, bias_out, g3, pre_one, g1):
    chan = params.shape[1]
    rows = MEL_ROWS
    wide = pre_two.shape[1]
    frame_dev = wide - RIM
    usable = masks[0:1]
    behind, ahead = (masks[n : n + 1].astype(BF16) for n in (1, 2))
    total = masks[3:4, 0:1]
    devices = payload.shape[0] // 14
    block = recv.shape[0] // devices
    pre_one[...] = dot(w1[2 * chan : (rows + 4) * chan], x3[...])

    def summed(k):
        return jnp.sum(recv[pl.ds(k, devices, stride=block), :], axis=0, keepdims=True)

    sums = summed(0)
    gain_sum, bias_sum = sums[:, :chan], sums[:, chan:]
    gain_out[...] = gain_sum
    bias_out[...] = bias_sum
    mean, inv = stats_two[0:chan, 0:1], stats_two[0:chan, 1:2]
    factor = to_column(params[2:3], chan) * inv
    gain_part = factor * (to_column(sums, chan) / total * inv)
    bias_part = factor * (to_column(sums, chan, chan) / total) - mean * gain_part
    gain_part = jnp.broadcast_to(gain_part, (chan, wide))
    bias_part = jnp.broadcast_to(bias_part, (chan, wide))
    factor = jnp.broadcast_to(factor, (chan, wide))
    scale = jnp.broadcast_to(stats[chan + 16 :, 0:1], (chan, wide))
    shift = jnp.broadcast_to(stats[chan + 16 :, 1:2], (chan, wide))
    factor_one = jnp.broadcast_to(to_column(params[0:1], chan) * stats[0:chan, 1:2], (chan, wide))
    count = pre_two.shape[0] // chan
    table = jnp.zeros((chan, 128), F32)
    for q in range(count):
        at = slice(q * chan, (q + 1) * chan)
        mask = usable if 0 <= q - 2 < rows else usable * row_valid(q - 2, rows)
        low = (factor * grad[at, :] - (bias_part + pre_two[at, :] * gain_part) * mask).astype(BF16)
        base = q * 3 * chan
        g3[base : base + chan, :], g3[base + 2 * chan : base + 3 * chan, :] = shifted_frames(low, behind, ahead)
        g3[base + chan : base + 2 * chan, :] = low
        if q < 3 or q % 2 == 0:
            continue
        start = q - 3
        result = dot(wb[...], g3[start * 3 * chan : (start + 4) * 3 * chan, :])
        for n in range(2):
            m = start + n - 1
            at = slice((m + 1) * chan, (m + 2) * chan)
            _, slope = silu_halves(pre_one[at, :] * scale + shift)
            mask = 0.5 * usable if 0 <= m < rows else usable * (0.5 * row_valid(m, rows))
            value = result[n * chan : (n + 1) * chan] * slope * mask
            out[at, :] = (value * factor_one).astype(BF16)
            if not 0 <= m < rows:
                continue
            g1[m * chan : (m + 1) * chan, :] = value[:, :frame_dev]
            if m % 4 == 3:
                part = g1[(m - 3) * chan : (m + 1) * chan, :]
                high = lax.reduce_precision(part, 8, 7)
                low = (part - high).astype(BF16)
                taps_in = x3[:, :frame_dev]
                products = dot(high.astype(BF16), taps_in, ((1,), (1,))) + dot(low, taps_in, ((1,), (1,)))
                for k in range(4):
                    table = table + pltpu.roll(products[k * chan : (k + 1) * chan], 128 - (m + k), 1)
    tap = iota((16, 128), 0)
    lane = iota((16, 128), 1)
    i = (tap * 11) >> 5
    select = ((lane == BAND * (tap - 3 * i) + i) & (tap < 9)) | ((lane == 3 * BAND) & (tap == 9))
    rows10 = dot(select.astype(F32), table, ((1,), (1,)), EXACT)
    share = block - 2
    mine = jnp.concatenate([summed(1 + k) for k in range(share)], axis=0)
    single = to_column(summed(block - 1), share)
    factor_l = params[2:3] * stats_two[chan : chan + 1, :chan]
    mine = mine[:, :chan] - (bias_sum * single + gain_sum * mine[:, chan:]) / total
    mine = factor_l * mine
    lower = -(-share // 2)
    mine = jnp.concatenate([mine] + [jnp.zeros((2 * lower - share, chan), F32)] * (share % 2), axis=0)
    mine = jnp.concatenate([mine[:lower], mine[lower:]], axis=1)
    if lower < 9:
        mine = jnp.concatenate([mine, jnp.zeros((9 - lower, 128), F32)], axis=0)
    sums = jnp.concatenate([rows10[0:5], rows10[5:10]], axis=1)
    block = jnp.concatenate([sums, mine], axis=0)
    for d in range(devices):
        payload[14 * d : 14 * (d + 1), :] = block


def transposed(low, w1, x3, stats, masks, ws_hbm, first, normed, ws, pre_one, sem):
    load = pltpu.make_async_copy(ws_hbm, ws, sem)
    load.start()
    chan = low.shape[0] // (MEL_ROWS + 2)
    wide = low.shape[1]
    pre_one[...] = dot(w1[2 * chan : (MEL_ROWS + 4) * chan], x3[...])
    mean = jnp.broadcast_to(stats[0:chan, 0:1], (chan, wide))
    inv = jnp.broadcast_to(stats[0:chan, 1:2], (chan, wide))
    for q in range(MEL_ROWS + 2):
        at = slice(q * chan, (q + 1) * chan)
        mask = masks[0:1] * row_valid(q - 1, MEL_ROWS)
        normed[at, :] = ((pre_one[at, :] - mean) * inv * mask).astype(BF16)
    load.wait()
    first[...] = dot(ws[...], low[...])


def finish(recv, features, stats, k1t, first, normed, ws, params, masks,
           spec_hbm, kernel_one_hbm, kernel_two_hbm, gain_hbm, bias_hbm,
           table, spec_grad, kernel_one, kernel_two, gain_out, bias_out, sems):
    chan = params.shape[1]
    rows = MEL_ROWS
    wide = normed.shape[1]
    frame_dev = wide - RIM
    usable, behind, ahead = (masks[n : n + 1] for n in range(3))
    total = masks[3:4, 0:1]
    gain = params[0:1]
    count = recv.shape[0] // 14
    share = -(-9 * chan // count)
    lower = -(-share // 2)
    left = [recv[pl.ds(5 + p, count, stride=14), :] for p in range(lower)]
    whole = jnp.concatenate([v[:, :chan] for v in left] + [v[:, chan:] for v in left], axis=0)
    for t in range(9):
        kernel_two[t] = whole[t * chan : (t + 1) * chan].T
    stores = [pltpu.make_async_copy(kernel_two, kernel_two_hbm, sems.at[3])]
    stores[0].start()
    sums = recv[0:5, :]
    for d in range(1, count):
        sums = sums + recv[14 * d : 14 * d + 5, :]
    ten = jnp.concatenate([sums[:, :chan], sums[:, chan:]], axis=0)
    bias_sum = ten[9:10]
    mean_l, inv_l = stats[chan : chan + 1, :chan], stats[chan + 8 : chan + 9, :chan]
    ten = ten - features[1:2, 0:1] * bias_sum
    k = k1t[0:9]
    gain_sum = inv_l * (jnp.sum(k * ten[0:9], axis=0, keepdims=True) - mean_l * bias_sum)
    gain_out[...] = gain_sum
    bias_out[...] = bias_sum
    for n, (source, target) in enumerate(((gain_out, gain_hbm), (bias_out, bias_hbm))):
        stores.append(pltpu.make_async_copy(source, target, sems.at[n]))
        stores[-1].start()
    factor_l = gain * inv_l
    scale = factor_l * gain_sum / total
    scale = jnp.concatenate([scale, scale], axis=1)
    scale = jnp.concatenate([scale] * ((rows + 2) // 2), axis=1)
    taps = first[...] - dot((ws[...].astype(F32) * scale).astype(BF16), normed[...])
    for part in range(wide // 128):
        table[part] = taps[:, 128 * part : 128 * (part + 1)]
    moved = [
        jnp.concatenate([table[part, pl.ds(b, rows, stride=8), :] for part in range(wide // 128)], axis=1)
        for b in range(3)
    ]
    constant = jnp.sum(k * (factor_l * bias_sum / total), axis=1, keepdims=True)
    for a in range(3):
        row = iota((rows, 1), 0) + (a - 1) + lax.axis_index("mel") * rows
        valid = ((row >= 0) & (row < lax.axis_size("mel") * rows)).astype(F32) * usable
        for b in range(3):
            t = 3 * (2 - a) + 2 - b
            moved[b] = moved[b] - constant[t : t + 1] * valid
    result = pltpu.roll(moved[0], 1, 1) * behind + moved[1] + pltpu.roll(moved[2], wide - 1, 1) * ahead
    spec_grad[0] = (result * usable)[:, :frame_dev]
    stores.append(pltpu.make_async_copy(spec_grad, spec_hbm, sems.at[2]))
    stores[-1].start()
    row = features[0:1, :]
    lane = iota((1, 128), 1)
    gram = jnp.concatenate(
        [jnp.where(lane < 9, pltpu.roll(row, 128 - 9 * t, 1) if t else row, 0.0) for t in range(9)]
        + [jnp.zeros((7, 128), F32)],
        axis=0,
    )
    single = to_column(row, 16, 81)[0:9]
    k_rows = jnp.concatenate([k1t[...], jnp.zeros((112, chan), F32)], axis=0)
    normed_taps = inv_l * (dot(gram, k_rows, precision=EXACT)[0:9] - single * mean_l)
    grad_taps = factor_l * (ten[0:9] - (bias_sum * single + gain_sum * normed_taps) / total)
    for i in range(3):
        kernel_one[i] = grad_taps[3 * i : 3 * i + 3]
    stores.append(pltpu.make_async_copy(kernel_one, kernel_one_hbm, sems.at[4]))
    stores[-1].start()
    for store in stores:
        store.wait()


def run(kernel, outs, scratch, *args, hbm=0, apart=(), flops=10**8, size=4 * 10**6):
    vmem = pl.BlockSpec(memory_space=pltpu.VMEM)
    specs = []
    args = list(args)
    for n, a in enumerate(args):
        if hbm and n >= len(args) - hbm:
            specs.append(pl.BlockSpec(memory_space=pltpu.HBM))
            args[n] = pltpu.with_memory_space_constraint(a, pltpu.HBM)
        else:
            specs.append(vmem)
            args[n] = pltpu.with_memory_space_constraint(a, pltpu.VMEM)
    return pl.pallas_call(
        kernel,
        out_shape=outs,
        in_specs=specs,
        out_specs=[pl.BlockSpec(memory_space=pltpu.HBM) if n in apart else vmem for n in range(len(outs))],
        scratch_shapes=scratch,
        compiler_params=pltpu.CompilerParams(vmem_limit_bytes=30 * 2**20),
        cost_estimate=pl.CostEstimate(flops=flops, bytes_accessed=size, transcendentals=0),
    )(*args)


def shape(dims, dtype=F32):
    return jax.ShapeDtypeStruct(dims, dtype)


def kept(dims, dtype=F32):
    return pltpu.VMEM(dims, dtype)


def far(dims, dtype=F32):
    return pltpu.HBM(dims, dtype)


def exchange(blocks, axes=AXES):
    return lax.all_to_all(blocks, axes, 0, 0, tiled=True)


def exchange_rows(rows, axes=AXES):
    return exchange(rows[:, None, :], axes)[:, 0, :]


def shards(spectrum, clip_bounds, kernel_one, gain_one, bias_one, kernel_two, gain_two, bias_two, pooled_grad):
    _, rows, frame_dev = spectrum.shape
    chan = kernel_two.shape[0]
    n_mel, n_tm = lax.axis_size("mel"), lax.axis_size("tm")
    devices = n_mel * n_tm
    half = frame_dev // 2
    wide = frame_dev + RIM
    mels = n_mel * rows

    packed, own, spec, masks = run(
        pack,
        [
            kept((devices, FIRST, 128), BF16),
            kept(pooled_grad.shape, BF16),
            kept(spectrum.shape, BF16),
            kept((8, wide)),
        ],
        [
            pltpu.SMEM(clip_bounds.shape, jnp.int32),
            pltpu.VMEM((2 * chan, half), F32),
            pltpu.VMEM((devices * FIRST, 128), F32),
            pltpu.SemaphoreType.DMA((3,)),
        ],
        spectrum,
        pooled_grad,
        clip_bounds,
        hbm=3,
    )
    recv = exchange(packed)
    ext = rows + 6
    span = 4 * 3 * chan
    wf, wb, w1, ws, pairs, singles, k1t, params, all_masks, edge_masks, twice, own_rows = run(
        weights,
        [
            kept((2 * chan, span), BF16),
            kept((2 * chan, span), BF16),
            kept((ext * chan, 128), BF16),
            far((rows * 8, (rows + 2) * chan), BF16),
            kept((chan, 128)),
            kept((chan, 128)),
            kept((16, chan)),
            kept((8, chan)),
            kept((8, n_tm * frame_dev)),
            kept((n_tm * 8, 128)),
            kept((128, 128)),
            kept((chan * rows // 2, half), BF16),
        ],
        [
            pltpu.VMEM((9, chan, chan), BF16),
            pltpu.VMEM((3, 3, chan), BF16),
            pltpu.VMEM((4, 1, chan), F32),
            pltpu.SMEM(clip_bounds.shape, jnp.int32),
            pltpu.VMEM((rows * 8, (rows + 2) * chan), BF16),
            pltpu.VMEM((chan * rows // 2, half), F32),
            pltpu.SemaphoreType.DMA((8,)),
        ],
        own,
        clip_bounds,
        jnp.transpose(kernel_two, (2, 3, 0, 1)).reshape(9, chan, chan),
        jnp.transpose(kernel_one, (1, 2, 0)),
        gain_one[None],
        bias_one[None],
        gain_two[None],
        bias_two[None],
        hbm=7,
        apart=(3,),
    )
    pre_two, payload, act, x3, stats_one, features = run(
        forward_one,
        [
            kept(((rows + 4) * chan, wide)),
            kept((devices, SECOND, 128), BF16),
            kept((ext * 3 * chan, wide), BF16),
            kept((128, wide), BF16),
            kept((2 * chan + 16, 128)),
            kept((8, 128)),
        ],
        [
            pltpu.VMEM((ext * chan, wide), F32),
            pltpu.VMEM((devices * FIRST, 128), F32),
            pltpu.VMEM((n_tm * 8, 128), F32),
            pltpu.VMEM((mels + 8, RIM), F32),
            pltpu.VMEM((devices * SECOND, 128), F32),
        ],
        recv,
        spec,
        pairs,
        singles,
        twice,
        w1,
        wf,
        params,
        masks,
        all_masks,
        edge_masks,
    )
    recv = exchange(payload)
    grad, payload, row_pairs, stats_two = run(
        backward_scaled,
        [
            kept(((rows + 4) * chan, wide)),
            kept((devices * sum_rows(devices, 9 * chan), 128)),
            far((rows // 2 * chan, frame_dev)),
            kept((chan + 8, 128)),
        ],
        [
            pltpu.VMEM(((rows // 2 + 2) * chan, RIM), F32),
            pltpu.VMEM((rows // 2 * chan, frame_dev), F32),
            pltpu.VMEM((3 * chan + 16, rows * frame_dev), BF16),
            pltpu.VMEM((devices * SECOND, 128), F32),
            pltpu.VMEM((2 * chan, half), F32),
            pltpu.SemaphoreType.DMA((rows // 4,)),
        ],
        recv,
        pre_two,
        act,
        own_rows,
        params,
        masks,
        apart=(2,),
    )
    recv = exchange_rows(payload)
    low, payload, gain_two_grad, bias_two_grad = run(
        backward,
        [
            kept(((rows + 2) * chan, wide), BF16),
            kept((devices * 14, 128)),
            shape((1, chan)),
            shape((1, chan)),
        ],
        [
            pltpu.VMEM(((rows + 4) * 3 * chan, wide), BF16),
            pltpu.VMEM(((rows + 2) * chan, wide), F32),
            pltpu.VMEM((rows * chan, frame_dev), F32),
        ],
        recv,
        pre_two,
        grad,
        stats_two,
        w1,
        x3,
        stats_one,
        params,
        masks,
        wb,
    )
    recv = exchange_rows(payload)
    (pooled,) = run(
        pool,
        [shape((1, chan, rows // 2, half), BF16)],
        [
            pltpu.VMEM((rows // 2 * chan, 128), F32),
            pltpu.VMEM((rows // 2 * chan, frame_dev), F32),
            pltpu.SemaphoreType.DMA,
        ],
        payload,
        row_pairs,
        hbm=1,
    )
    first, normed, ws = run(
        transposed,
        [
            kept((rows * 8, wide)),
            kept(((rows + 2) * chan, wide), BF16),
            kept((rows * 8, (rows + 2) * chan), BF16),
        ],
        [pltpu.VMEM(((rows + 2) * chan, wide), F32), pltpu.SemaphoreType.DMA],
        low,
        w1,
        x3,
        stats_one,
        masks,
        ws,
        hbm=1,
    )
    spec_grad, kernel_one_grad, kernel_two_grad, gain_one_grad, bias_one_grad = run(
        finish,
        [
            shape((1, rows, frame_dev)),
            shape((3, 3, chan)),
            shape((9, chan, chan)),
            shape((1, chan)),
            shape((1, chan)),
        ],
        [
            pltpu.VMEM((3, rows * 8, 128), F32),
            pltpu.VMEM((1, rows, frame_dev), F32),
            pltpu.VMEM((3, 3, chan), F32),
            pltpu.VMEM((9, chan, chan), F32),
            pltpu.VMEM((1, chan), F32),
            pltpu.VMEM((1, chan), F32),
            pltpu.SemaphoreType.DMA((5,)),
        ],
        recv,
        features,
        stats_one,
        k1t,
        first,
        normed,
        ws,
        params,
        masks,
        apart=range(5),
    )
    kernel_two_grad = jnp.transpose(kernel_two_grad.reshape(3, 3, chan, chan), (2, 3, 0, 1))
    return (
        pooled,
        spec_grad,
        jnp.transpose(kernel_one_grad, (2, 0, 1)),
        gain_one_grad[0],
        bias_one_grad[0],
        kernel_two_grad,
        gain_two_grad[0],
        bias_two_grad[0],
    )


def solution(mesh):
    return jax.shard_map(
        shards,
        mesh=mesh,
        in_specs=(
            P(None, "mel", "tm"),
            P(),
            P(),
            P(),
            P(),
            P(),
            P(),
            P(),
            P(None, None, "mel", "tm"),
        ),
        out_specs=(P(None, None, "mel", "tm"), P(None, "mel", "tm"), P(), P(), P(), P(), P(), P()),
        check_vma=False,
    )
```

```python
import math

import jax
import jax.numpy as jnp
from jax import lax
from jax.experimental import pallas as pl
from jax.experimental.pallas import tpu as pltpu
from jax.sharding import PartitionSpec as P

F32 = jnp.float32
BF16 = jnp.bfloat16
AXES = ("mel", "tm")
EXACT = lax.Precision.HIGHEST
RIM = 128
BAND = 24
MEL_ROWS = 16
FIRST = 24
SUMS, EDGES, COLUMNS = 16, 19, 23
SIDE = 96
SECOND = 8


def iota(shape, dim):
    return lax.broadcasted_iota(jnp.int32, shape, dim)


def dot(a, b, over=((1,), (0,)), precision=None):
    return lax.dot_general(a, b, (over, ((), ())), precision=precision, preferred_element_type=F32)


def to_column(lanes, count, start=0):
    shape = (count, lanes.shape[1])
    return jnp.sum(jnp.where(iota(shape, 1) == iota(shape, 0) + start, lanes, 0.0), axis=1, keepdims=True)


def to_lanes(column, start=0, width=128):
    shape = (column.shape[0], width)
    return jnp.sum(jnp.where(iota(shape, 1) == iota(shape, 0) + start, column, 0.0), axis=0, keepdims=True)


def halves(v):
    total = v[:, :128]
    for n in range(128, v.shape[1], 128):
        total = total + v[:, n : n + 128]
    return total


def frame_masks(bounds, frames):
    last = bounds.shape[1] - 1

    def living(f):
        return (f >= 0) & (f < bounds[0, last])

    def paired(f):
        both = living(f) & living(f + 1)
        for k in range(1, last):
            both = both & (f + 1 != bounds[0, k])
        return both

    return tuple(m.astype(F32) for m in (living(frames), paired(frames - 1), paired(frames)))


def row_valid(row, rows):
    mel = lax.axis_index("mel") * rows + row
    return ((mel >= 0) & (mel < lax.axis_size("mel") * rows)).astype(F32)


def start_all(*pairs, sems):
    copies = [pltpu.make_async_copy(src, dst, sems.at[n]) for n, (src, dst) in enumerate(pairs)]
    for copy in copies:
        copy.start()
    return copies


def wait_all(copies):
    for copy in copies:
        copy.wait()


def shifted_frames(value, behind, ahead):
    wide = value.shape[1]
    return pltpu.roll(value, 1, 1) * behind, pltpu.roll(value, wide - 1, 1) * ahead


def three_parts(v):
    high = lax.reduce_precision(v, 8, 7)
    mid = lax.reduce_precision(v - high, 8, 7)
    return high, mid, v - high - mid


def share_of(devices, chan):
    return -(-chan // devices)


def pack(spec_hbm, grad_hbm, bounds_hbm, out, own, spec, masks, bounds, edges, rows_out, sems):
    copies = start_all((bounds_hbm, bounds), (spec_hbm, spec), (grad_hbm, own), sems=sems)
    copies[0].wait()
    wide = masks.shape[1]
    frame_dev = wide - RIM
    devices = out.shape[0]
    rows = MEL_ROWS
    lane = iota((1, wide), 1)
    frames = lax.axis_index("tm") * frame_dev + jnp.where(lane < frame_dev + RIM // 2, lane, lane - wide)
    last = bounds.shape[1] - 1
    pixels = (bounds[0, last] * (lax.axis_size("mel") * rows)).astype(F32)
    found = frame_masks(bounds, frames)
    masks[...] = jnp.concatenate(
        list(found) + [jnp.full((1, wide), 1.0) * pixels, jnp.zeros((4, wide), F32)], axis=0
    )
    usable, behind, ahead = (m[:, :frame_dev] for m in found)
    copies[1].wait()
    x = spec[0].astype(F32) * usable
    lane = iota((1, frame_dev), 1)
    row = iota((rows, 1), 0)
    inner = jnp.where((lane > 0) & (lane < frame_dev - 1), usable, 0.0)
    number = (rows - 2) * jnp.sum(inner, axis=1, keepdims=True)
    inner = inner * ((row > 0) & (row < rows - 1)).astype(F32)
    centre = jnp.sum(jnp.sum(x, axis=0, keepdims=True), axis=1, keepdims=True)
    centre = centre / (rows * jnp.maximum(jnp.sum(usable, axis=1, keepdims=True), 1.0))
    centre = lax.reduce_precision(centre, 8, 7)
    shifted = [pltpu.roll(x, 1, 1) * behind, x, pltpu.roll(x, frame_dev - 1, 1) * ahead]
    taps = [pltpu.roll(v, (1 - i) % rows, 0) if i != 1 else v for i in range(3) for v in shifted]
    features = feature_rows(centre, (taps, inner))
    lane = iota((1, 128), 1)
    features = jnp.where(lane == 90, centre, jnp.where(lane == 91, number, features))
    pick = iota((8, frame_dev), 0)
    column = jnp.where(pick < 4, pick, frame_dev - 8 + pick)
    strip = dot((iota((8, frame_dev), 1) == column).astype(BF16), x.astype(BF16), ((1,), (1,)))
    lane = iota((8, 128), 1)
    repeat = (iota((rows, 128), 1) % rows == iota((rows, 128), 0)).astype(BF16)
    strip = jnp.where(lane // rows == iota((8, 128), 0), dot(strip.astype(BF16), repeat), 0.0)
    strip = jnp.sum(strip, axis=0, keepdims=True)

    def put(n, value):
        rows_out[pl.ds(n, devices, stride=FIRST), :] = jnp.broadcast_to(value, (devices, 128))

    near = jnp.concatenate([x[0:4], x[rows - 4 :]], axis=0)
    for n in range(8):
        put(n, near[n : n + 1, :128])
        put(8 + n, near[n : n + 1, 128:])
    put(COLUMNS, strip)
    copies[2].wait()
    _, chan, many, half = own.shape
    share = share_of(devices, chan)
    holders = chan // share
    g = own[0].astype(F32)
    edges[0:chan] = g[:, 0, :]
    edges[chan:] = g[:, many - 1, :]

    def spread_out(v):
        if holders < devices:
            v = jnp.concatenate([v, jnp.zeros((devices - holders, 128), F32)], axis=0)
        return v

    for n in range(share):
        put(EDGES + n, spread_out(edges[n * holders : (n + 1) * holders, :]))
        put(EDGES + share + n, spread_out(edges[chan + n * holders : chan + (n + 1) * holders, :]))
    for n in range(2 * share, COLUMNS - EDGES):
        put(EDGES + n, jnp.zeros((1, 128), F32))
    end = iota((8, half), 0)
    at = iota((8, half), 1)
    ends = ((end == 0) & (at == 0)) | ((end == 1) & (at == half - 1))
    columns = dot(ends.astype(BF16), g.reshape(chan * many, half).astype(BF16), ((1,), (1,)))
    group = 128 // many
    source = iota((128, 128), 0)
    lane = iota((group, 128), 1)
    mine = lane // many == iota((group, 128), 0)
    parts = three_parts(features)
    for n in range(2):
        side = jnp.zeros((holders, 128), F32)
        for m in range(share):
            move = (iota((128, 128), 1) == SIDE + many * m + source % many).astype(BF16)
            first = m * holders * many // 128
            block = [columns[n : n + 1, 128 * q : 128 * (q + 1)] for q in range(first, first + holders * many // 128)]
            block = jnp.concatenate([jnp.where(mine, v, 0.0) for v in block], axis=0)
            side = side + dot(block.astype(BF16), move)
        put(SUMS + n, spread_out(side) + parts[n])
    put(SUMS + 2, parts[2])
    out[...] = rows_out[...].reshape(out.shape).astype(BF16)


def weights(own, bounds_hbm, k2_hbm, k1_hbm, gain_one_hbm, bias_one_hbm, gain_two_hbm, bias_two_hbm,
            wf, wb, w1, ws_hbm, pairs, singles, k1t, params, all_masks, edge_masks, twice, own_rows,
            k2, k1, vectors, bounds, ws, temp, sems):
    loads = start_all(
        (bounds_hbm, bounds),
        (k2_hbm, k2),
        (k1_hbm, k1),
        (gain_one_hbm, vectors.at[0]),
        (bias_one_hbm, vectors.at[1]),
        (gain_two_hbm, vectors.at[2]),
        (bias_two_hbm, vectors.at[3]),
        sems=sems,
    )
    _, many, count, half = own.shape
    temp[...] = own[0].astype(F32).reshape(many * count, half)
    for r in range(count):
        own_rows[r * many : (r + 1) * many] = temp[pl.ds(r, many, stride=count), :].astype(BF16)
    wait_all(loads)
    chan = k2.shape[1]
    span = wf.shape[1]
    taps = [k2[t].astype(F32) for t in range(9)]
    rest = jnp.zeros((chan, span - 9 * chan), F32)
    forward = jnp.concatenate(taps + [rest], axis=1)
    backward = jnp.concatenate([taps[8 - t].T for t in range(9)] + [rest], axis=1)
    for r in range(wb.shape[0] // chan):
        at = slice(r * chan, (r + 1) * chan)
        wb[at] = (pltpu.roll(backward, 3 * chan * r, 1) if r else backward).astype(BF16)
    full = jnp.concatenate([k1[n].astype(F32) for n in range(3)] + [jnp.zeros((7, chan), F32)], axis=0)
    low = [
        jnp.concatenate([full[3 * (2 - a) + 2 - b : 3 * (2 - a) + 3 - b] for a in range(3)], axis=1)
        for b in range(3)
    ]
    base = jnp.concatenate(low + [jnp.zeros((5, 3 * chan), F32)], axis=0)
    base = jnp.concatenate([base, jnp.zeros((8, ws.shape[1] - 3 * chan), F32)], axis=1)
    for m in range(ws.shape[0] // 8):
        ws[8 * m : 8 * m + 8] = (pltpu.roll(base, chan * m, 1) if m else base).astype(BF16)
    store_ws = pltpu.make_async_copy(ws, ws_hbm, sems.at[7])
    store_ws.start()
    frames = all_masks.shape[1]
    frame_dev = frames // lax.axis_size("tm")
    all_masks[...] = jnp.concatenate(
        list(frame_masks(bounds, iota((1, frames), 1))) + [jnp.zeros((5, frames), F32)], axis=0
    )
    q = iota(edge_masks.shape, 0)
    lane = iota(edge_masks.shape, 1)
    k = q % 8
    frames = (q // 8) * frame_dev + jnp.where(k < 4, k, k + frame_dev - 8)
    living, behind, ahead = frame_masks(bounds, frames)
    living = jnp.where((k == 0) | (k == 7), living, 0.0)
    edge_masks[...] = jnp.where(lane == 0, living, jnp.where(lane == 1, behind, jnp.where(lane == 2, ahead, 0.0)))
    params[...] = jnp.concatenate(
        [vectors[n] for n in range(4)] + [jnp.zeros((4, chan), F32)], axis=0
    )
    tap = iota((16, 128), 0)
    lane = iota((16, 128), 1)
    i = (tap * 11) >> 5
    ninth = (lane * 57) >> 9
    to_band = (lane == BAND * (tap - 3 * i) + i) & (tap < 9)
    to_left = (ninth == tap) & (tap < 9)
    to_right = (lane - 9 * ninth == tap) & (lane < 81)
    to_single = (lane == 81 + tap) & (tap < 9)
    source = iota((128, 128), 0) - 81
    lane = iota((128, 128), 1)
    ninth = (lane * 57) >> 9
    inside = (source >= 0) & (source < 9) & (lane < 81)
    twice[...] = jnp.where(inside, (source == ninth).astype(F32) + (source == lane - 9 * ninth).astype(F32), 0.0)
    for r in range(wf.shape[0] // chan):
        at = slice(r * chan, (r + 1) * chan)
        wf[at] = (pltpu.roll(forward, 3 * chan * r, 1) if r else forward).astype(BF16)
    k1t[...] = full
    k = full.astype(BF16)
    lanes = [dot(k, select.astype(BF16), ((0,), (0,))) for select in (to_band, to_left, to_right, to_single)]
    pairs[...] = lanes[1] * lanes[2]
    singles[...] = lanes[3]
    for m in range(w1.shape[0] // chan):
        w1[m * chan : (m + 1) * chan] = (pltpu.roll(lanes[0], m, 1) if m else lanes[0]).astype(BF16)
    store_ws.wait()


def feature_rows(centre, *parts):
    def folded(v):
        return jnp.sum(halves(v), axis=0, keepdims=True)

    rows = [jnp.zeros((1, 128), F32)] * 96
    for taps, weight in parts:
        z = [tap - centre for tap in taps]
        for s in range(9):
            left = z[s] * weight
            rows[81 + s] = rows[81 + s] + folded(left)
            for t in range(s, 9):
                rows[9 * s + t] = rows[9 * t + s] = rows[9 * s + t] + folded(left * z[t])
    return to_lanes(jnp.sum(jnp.concatenate(rows, axis=0), axis=1, keepdims=True))


def summed_blocks(ref, devices):
    block = ref.shape[0] // devices
    period = 8 // math.gcd(block, 8)
    step = period * block
    total = ref[0:step, :]
    for at in range(step, ref.shape[0], step):
        total = total + ref[at : at + step, :]
    result = total[0:block]
    for n in range(1, period):
        result = result + total[n * block : (n + 1) * block]
    return result


def moved_rows(v, step):
    if step == 0:
        return v
    count = v.shape[0]
    if abs(step) >= count:
        return jnp.zeros_like(v)
    zero = jnp.zeros((abs(step), v.shape[1]), v.dtype)
    if step > 0:
        return jnp.concatenate([zero, v[: count - step]], axis=0)
    return jnp.concatenate([v[-step:], zero], axis=0)


def silu_halves(h):
    t = jnp.tanh(h)
    one = 1.0 + t
    return h * one, one * (1.0 + h * (1.0 - t))


def forward_one(recv, spec, pairs, singles, twice, w1, wf, params, masks, all_masks, edge_masks,
                pre_two, payload, act, x3, stats, features_out, pre_one, got, strips, halo, rows_out):
    devices = recv.shape[0]
    n_mel, count = lax.axis_size("mel"), lax.axis_size("tm")
    rows = MEL_ROWS
    mels = n_mel * rows
    wide = masks.shape[1]
    frame_dev = wide - RIM
    chan = params.shape[1]
    me_m, me_t = lax.axis_index("mel"), lax.axis_index("tm")
    usable, behind, ahead = (masks[n : n + 1] for n in range(3))
    total = masks[3:4, 0:1]
    got[...] = recv[...].astype(F32).reshape(devices * FIRST, 128)

    def every(n):
        return got[pl.ds(n, devices, stride=FIRST), :]

    lane = iota((count, 128), 1)
    bands = [got[pl.ds(FIRST * k * count + COLUMNS, count, stride=FIRST), :] for k in range(n_mel)]
    for c in range(8):
        column = jnp.zeros((count, 128), F32)
        for k, band in enumerate(bands):
            part = jnp.where(lane // rows == c, band, 0.0)
            column = column + (pltpu.roll(part, rows * (k - c) % 128, 1) if k != c else part)
        strips[pl.ds(c, count, stride=8), :] = column
    at = pl.multiple_of(FIRST * (jnp.maximum(me_m - 1, 0) * count + me_t), 8)
    above = got[pl.ds(at, 16), :] * (me_m > 0).astype(F32)
    at = pl.multiple_of(FIRST * (jnp.minimum(me_m + 1, n_mel - 1) * count + me_t), 8)
    below = got[pl.ds(at, 16), :] * (me_m < n_mel - 1).astype(F32)
    above = jnp.concatenate([above[4:8], above[12:16]], axis=1)
    below = jnp.concatenate([below[0:4], below[8:12]], axis=1)
    own = spec[0].astype(F32) * usable[:, :frame_dev]
    at = pl.multiple_of(8 * jnp.minimum(me_t + 1, count - 1), 8)
    after = strips[pl.ds(at, 8), :][:, :mels] * (me_t + 1 < count).astype(F32)
    at = pl.multiple_of(8 * jnp.maximum(me_t - 1, 0), 8)
    before = strips[pl.ds(at, 8), :][:, :mels] * (me_t > 0).astype(F32)
    sides = jnp.concatenate([after[0:4], before[4:8], jnp.zeros((8, mels), F32)], axis=0).astype(BF16)
    side = iota((16, RIM), 0)
    place = iota((16, RIM), 1) == jnp.where(side < 4, side, jnp.where(side < 8, side + RIM - 8, -1))
    halo[0:8] = jnp.zeros((8, RIM), F32)
    halo[mels : mels + 8] = jnp.zeros((8, RIM), F32)
    halo[4 : mels + 4] = dot(sides, place.astype(BF16), ((0,), (0,)))
    rim = halo[pl.ds(pl.multiple_of(me_m * rows, 8), BAND), :]
    near = jnp.concatenate([jnp.concatenate([above, own, below], axis=0), rim], axis=1)
    x3[...] = jnp.concatenate(
        [
            pltpu.roll(near, 1, 1) * behind,
            near,
            pltpu.roll(near, wide - 1, 1) * ahead,
            jnp.broadcast_to(usable, (BAND, wide)),
            jnp.zeros((128 - 4 * BAND, wide), F32),
        ],
        axis=0,
    ).astype(BF16)
    pre_one[...] = dot(w1[...], x3[...])
    lane = iota((1, 128), 1)
    parts = jnp.where(lane < 92, every(SUMS) + every(SUMS + 1) + every(SUMS + 2), 0.0)
    centres, numbers = parts[:, 90:91], parts[:, 91:92]
    centre = jnp.sum(centres * numbers, axis=0, keepdims=True)
    centre = centre / jnp.maximum(jnp.sum(numbers, axis=0, keepdims=True), 1.0)
    delta = centres - centre
    features = jnp.sum(parts + delta * numbers * jnp.where(lane < 81, delta, 1.0), axis=0, keepdims=True)
    moved = jnp.sum(delta * parts, axis=0, keepdims=True)
    moved = dot(jnp.broadcast_to(moved, (8, 128)), twice[...], precision=EXACT)[0:1]
    features = features + moved
    tiles = []
    for k in range(n_mel):
        lanes = []
        for d in range(count):
            at = FIRST * (k * count + d)
            lanes += [got[at : at + 8, :], got[at + 8 : at + 16, :]]
        tiles.append(jnp.concatenate(lanes, axis=1))
    zero = jnp.zeros((1, tiles[0].shape[1]), F32)
    before_row, this_row, next_row = [], [], []
    for k, tile in enumerate(tiles):
        before_row += [tiles[k - 1][7:8] if k else zero, tile[6:7]]
        this_row += [tile[0:1], tile[7:8]]
        next_row += [tile[1:2], tiles[k + 1][0:1] if k + 1 < n_mel else zero]
    f_usable, f_behind, f_ahead = (all_masks[n : n + 1] for n in range(3))
    taps = []
    for group in (before_row, this_row, next_row):
        v = jnp.concatenate(group, axis=0)
        taps += [pltpu.roll(v, 1, 1) * f_behind, v, pltpu.roll(v, v.shape[1] - 1, 1) * f_ahead]
    borders = (taps, f_usable)
    edge = strips[...]
    q_usable, q_behind, q_ahead = (edge_masks[:, n : n + 1] for n in range(3))
    lane = iota((count * 8, 128), 1)
    inside = (lane < mels) & (lane % rows != 0) & (lane % rows != rows - 1)
    shifted = [
        pltpu.roll(edge, 1, 0) * q_behind,
        edge,
        pltpu.roll(edge, count * 8 - 1, 0) * q_ahead,
    ]
    taps = [pltpu.roll(v, (1 - i) % 128, 1) if i != 1 else v for i in range(3) for v in shifted]
    features = features + feature_rows(centre, borders, (taps, jnp.where(inside, q_usable, 0.0)))
    features = jnp.where(iota((1, 128), 1) < 90, features, 0.0)
    features_out[...] = jnp.concatenate(
        [features, jnp.broadcast_to(centre, (1, 128)), jnp.zeros((6, 128), F32)], axis=0
    )
    near_mean = jnp.sum(singles[...] * features, axis=1, keepdims=True) / total
    square = jnp.sum(pairs[...] * features, axis=1, keepdims=True) / total
    inv = lax.rsqrt(square - near_mean * near_mean + 1e-05)
    mean = near_mean + centre * jnp.sum(singles[...], axis=1, keepdims=True)
    lane = iota((chan, 128), 1)
    stats[0:chan] = jnp.where(lane == 0, mean, jnp.where(lane == 1, inv, 0.0))
    stats[chan : chan + 8] = jnp.broadcast_to(to_lanes(near_mean), (8, 128))
    stats[chan + 8 : chan + 16] = jnp.broadcast_to(to_lanes(inv), (8, 128))
    scale = 0.5 * to_column(params[0:1], chan) * inv
    shift = 0.5 * to_column(params[1:2], chan) - mean * scale
    stats[chan + 16 :] = jnp.where(lane == 0, scale, jnp.where(lane == 1, shift, 0.0))
    scale = jnp.broadcast_to(scale, (chan, wide))
    shift = jnp.broadcast_to(shift, (chan, wide))
    ext = w1.shape[0] // chan
    block, taps = wf.shape
    first = jnp.zeros((chan, 128), F32)
    second = jnp.zeros((chan, 128), F32)
    own_mask = usable[:, :frame_dev]
    low_masks = [m.astype(BF16) for m in (usable, behind, ahead)]
    for r in range(ext):
        value, _ = silu_halves(pre_one[r * chan : (r + 1) * chan, :] * scale + shift)
        if not 0 <= r - 3 < rows:
            value = value * row_valid(r - 3, rows)
        base = r * 3 * chan
        low = value.astype(BF16) * low_masks[0]
        act[base : base + chan, :], act[base + 2 * chan : base + 3 * chan, :] = shifted_frames(low, *low_masks[1:])
        act[base + chan : base + 2 * chan, :] = low
        if r < 3 or r % 2 == 0:
            continue
        g = (r - 3) // 2
        result = dot(wf[...], act[g * 3 * block : g * 3 * block + taps, :])
        pre_two[g * block : (g + 1) * block] = result
        for q in range(2):
            if 2 <= 2 * g + q < rows + 2:
                p = result[q * chan : (q + 1) * chan, :frame_dev]
                masked = p * own_mask
                first = first + halves(masked)
                second = second + halves(masked * p)
    share = share_of(devices, chan)

    def put(n, value):
        rows_out[pl.ds(n, devices, stride=SECOND), :] = jnp.broadcast_to(value, (devices, 128))

    for n in range(share):
        put(3 + n, moved_rows(every(EDGES + share + n), count))
        put(3 + share + n, moved_rows(every(EDGES + n), -count))
    for n in range(3 + 2 * share, SECOND - 1):
        put(n, jnp.zeros((1, 128), F32))
    lane = iota((devices, 128), 1)
    tm = iota((devices, 128), 0) % count
    lefts = jnp.where(lane >= SIDE, every(SUMS), 0.0)
    rights = jnp.where(lane >= SIDE, every(SUMS + 1), 0.0)
    beside = jnp.zeros((devices, 128), F32)
    for n, step in enumerate((0, count, -count)):
        one = jnp.where(tm > 0, moved_rows(rights, step + 1), 0.0)
        two = jnp.where(tm < count - 1, moved_rows(lefts, step - 1), 0.0)
        beside = beside + pltpu.roll(one, (32 * n - SIDE) % 128, 1) + pltpu.roll(two, (32 * n + 16 - SIDE) % 128, 1)
    put(SECOND - 1, beside)
    first = jnp.sum(first, axis=1, keepdims=True)
    second = jnp.sum(second, axis=1, keepdims=True)
    for n, part in enumerate(three_parts(to_lanes(first) + to_lanes(second, chan))):
        put(n, part)
    payload[...] = rows_out[...].reshape(payload.shape).astype(BF16)


def sum_rows(devices, taps):
    return -(-taps // devices) + 2


def backward_scaled(recv, pre_two, act, own_rows, params, masks,
                    grad, payload, stats, sides, right, got, beyond):
    devices = recv.shape[0]
    got[...] = recv[...].astype(F32).reshape(devices * SECOND, 128)
    chan = params.shape[1]
    half = own_rows.shape[1]
    lane = iota((half, 2 * half), 1)
    spread = jnp.where(lane >> 1 == iota((half, 2 * half), 0), 0.25, 0.0).astype(BF16)
    rows = MEL_ROWS
    wide = pre_two.shape[1]
    frame_dev = wide - RIM
    usable = masks[0:1]
    share = share_of(devices, chan)
    holders = chan // share

    def every(n):
        return got[pl.ds(n, devices, stride=SECOND), :]

    beside = every(SECOND - 1)[:holders]
    lane = iota((holders, RIM), 1)
    many = rows // 2
    for n in range(share):
        first = n * holders
        beyond[first : first + holders, :] = every(3 + n)[:holders]
        beyond[chan + first : chan + first + holders, :] = every(3 + share + n)[:holders]
        for r in range(many + 2):
            at = many * n + (r if r < many else 32 + many - 1 if r == many else 64)
            left, right_of = beside[:, at : at + 1], beside[:, at + 16 : at + 17]
            side = jnp.where(lane >= RIM - 2, 0.25 * left, jnp.where(lane < 2, 0.25 * right_of, 0.0))
            sides[r * chan + first : r * chan + first + holders, :] = side
    total = masks[3:4, 0:1]
    sums = jnp.sum(every(0) + every(1) + every(2), axis=0, keepdims=True)
    mean = to_column(sums, chan) / total
    inv = lax.rsqrt(to_column(sums, chan, chan) / total - mean * mean + 1e-05)
    lane = iota((chan, 128), 1)
    scale = 0.5 * to_column(params[2:3], chan) * inv
    shift = 0.5 * to_column(params[3:4], chan) - mean * scale
    columns = jnp.zeros((chan, 128), F32)
    for n, column in enumerate((mean, inv, scale, shift)):
        columns = jnp.where(lane == n, column, columns)
    stats[0:chan] = columns
    stats[chan : chan + 8] = jnp.broadcast_to(to_lanes(inv), (8, 128))
    shift = jnp.broadcast_to(shift, (chan, wide))
    scale = jnp.broadcast_to(scale, (chan, wide))
    mean = jnp.broadcast_to(mean, (chan, frame_dev))
    inv = jnp.broadcast_to(inv, (chan, frame_dev))
    first = jnp.zeros((chan, 128), F32)
    second = jnp.zeros((chan, 128), F32)
    right[3 * chan :] = jnp.ones((16, rows * frame_dev), BF16)
    table = jnp.zeros((9 * chan, 3 * chan + 16), F32)
    for q in list(range(2, rows + 2)) + [0, 1, rows + 2, rows + 3]:
        r = q // 2
        at = slice(q * chan, (q + 1) * chan)
        m = q - 2
        mask = 0.5 * usable if 0 <= m < rows else usable * (0.5 * row_valid(m, rows))
        if q % 2 == 0:
            if 1 <= r <= rows // 2:
                pooled, at_side = own_rows[(r - 1) * chan : r * chan], (r - 1) * chan
            elif r == 0:
                pooled, at_side = beyond[0:chan].astype(BF16), many * chan
            else:
                pooled, at_side = beyond[chan:].astype(BF16), (many + 1) * chan
            up = jnp.concatenate([dot(pooled, spread), sides[at_side : at_side + chan, :]], axis=1)
        pre = pre_two[at, :]
        _, slope = silu_halves(pre * scale + shift)
        g = up * slope * mask
        grad[at, :] = g
        if not 0 <= m < rows:
            continue
        g = g[:, :frame_dev]
        normed = (pre[:, :frame_dev] - mean) * inv
        first = first + halves(g * normed)
        second = second + halves(g)
        lanes = slice(m * frame_dev, (m + 1) * frame_dev)
        high = lax.reduce_precision(g, 8, 7)
        right[0:chan, lanes] = high.astype(BF16)
        right[chan : 2 * chan, lanes] = (g - high).astype(BF16)
        right[2 * chan : 3 * chan, lanes] = normed.astype(BF16)
        if m % 4 == 3:
            left = [act[(n + 2) * 3 * chan : (n + 5) * 3 * chan, :frame_dev] for n in range(m - 3, m + 1)]
            lanes = slice((m - 3) * frame_dev, (m + 1) * frame_dev)
            table = table + dot(jnp.concatenate(left, axis=1), right[:, lanes], ((1,), (1,)))
    first = jnp.sum(first, axis=1, keepdims=True)
    second = jnp.sum(second, axis=1, keepdims=True)
    totals = to_lanes(first) + to_lanes(second, chan)
    block = payload.shape[0] // devices
    payload[pl.ds(0, devices, stride=block), :] = jnp.broadcast_to(totals, (devices, 128))
    both = jnp.concatenate([table[:, :chan] + table[:, chan : 2 * chan], table[:, 2 * chan : 3 * chan]], axis=1)
    single = table[:, 3 * chan : 3 * chan + 1]
    lane = iota((devices, 128), 1)
    constants = jnp.zeros((devices, 128), F32)
    for k in range(block - 2):
        cut, ones = both[k * devices : (k + 1) * devices], single[k * devices : (k + 1) * devices]
        short = devices - cut.shape[0]
        if short:
            cut = jnp.concatenate([cut, jnp.zeros((short, 128), F32)], axis=0)
            ones = jnp.concatenate([ones, jnp.zeros((short, 1), F32)], axis=0)
        payload[pl.ds(1 + k, devices, stride=block), :] = cut
        constants = jnp.where(lane == k, ones, constants)
    payload[pl.ds(block - 1, devices, stride=block), :] = constants


def pool(after, stats, masks, pre_hbm, out, temp, pre_two, sems):
    del after
    chan, rows, half = out.shape[1:]
    frame_dev = 2 * half
    loads = start_all(*((pre_hbm.at[r], pre_two.at[r]) for r in range(rows)), sems=sems)
    to_mean = jnp.where(iota((frame_dev, half), 0) >> 1 == iota((frame_dev, half), 1), 0.25, 0.0)
    usable = masks[0:1, :frame_dev]
    scale = jnp.broadcast_to(stats[0:chan, 2:3], (chan, frame_dev))
    shift = jnp.broadcast_to(stats[0:chan, 3:4], (chan, frame_dev))
    for r in range(rows):
        loads[r].wait()
        both = [silu_halves(pre_two[r, h * chan : (h + 1) * chan, :] * scale + shift)[0] * usable for h in range(2)]
        temp[pl.ds(r, chan, stride=rows), :] = dot(both[0] + both[1], to_mean, precision=EXACT)
    out[0] = temp[...].reshape(chan, rows, half).astype(BF16)


def backward(recv, pre_two, grad, stats_two, w1, x3, stats, params, masks, wb,
             out, payload, gain_out, bias_out, pre_hbm, g3, pre_one, g1, sems):
    chan = params.shape[1]
    rows = MEL_ROWS
    wide = pre_two.shape[1]
    frame_dev = wide - RIM
    usable = masks[0:1]
    behind, ahead = (masks[n : n + 1].astype(BF16) for n in (1, 2))
    total = masks[3:4, 0:1]
    devices = payload.shape[0] // 14
    stores = start_all(
        *(
            (pre_two.at[pl.ds(2 * (r + 1) * chan, 2 * chan), pl.ds(0, frame_dev)], pre_hbm.at[r])
            for r in range(rows // 2)
        ),
        sems=sems,
    )
    pre_one[...] = dot(w1[2 * chan : (rows + 4) * chan], x3[...])

    received = summed_blocks(recv, devices)
    sums = received[0:1]
    gain_sum, bias_sum = sums[:, :chan], sums[:, chan:]
    gain_out[...] = gain_sum
    bias_out[...] = bias_sum
    mean, inv = stats_two[0:chan, 0:1], stats_two[0:chan, 1:2]
    factor = to_column(params[2:3], chan) * inv
    gain_part = factor * (to_column(sums, chan) / total * inv)
    bias_part = factor * (to_column(sums, chan, chan) / total) - mean * gain_part
    gain_part = jnp.broadcast_to(gain_part, (chan, wide))
    bias_part = jnp.broadcast_to(bias_part, (chan, wide))
    factor = jnp.broadcast_to(factor, (chan, wide))
    scale = jnp.broadcast_to(stats[chan + 16 :, 0:1], (chan, wide))
    shift = jnp.broadcast_to(stats[chan + 16 :, 1:2], (chan, wide))
    factor_one = jnp.broadcast_to(to_column(params[0:1], chan) * stats[0:chan, 1:2], (chan, wide))
    count = pre_two.shape[0] // chan
    table = jnp.zeros((chan, 128), F32)
    for q in range(count):
        at = slice(q * chan, (q + 1) * chan)
        mask = usable if 0 <= q - 2 < rows else usable * row_valid(q - 2, rows)
        low = (factor * grad[at, :] - (bias_part + pre_two[at, :] * gain_part) * mask).astype(BF16)
        base = q * 3 * chan
        g3[base : base + chan, :], g3[base + 2 * chan : base + 3 * chan, :] = shifted_frames(low, behind, ahead)
        g3[base + chan : base + 2 * chan, :] = low
        if q < 3 or q % 2 == 0:
            continue
        start = q - 3
        result = dot(wb[...], g3[start * 3 * chan : (start + 4) * 3 * chan, :])
        for n in range(2):
            m = start + n - 1
            at = slice((m + 1) * chan, (m + 2) * chan)
            _, slope = silu_halves(pre_one[at, :] * scale + shift)
            mask = 0.5 * usable if 0 <= m < rows else usable * (0.5 * row_valid(m, rows))
            value = result[n * chan : (n + 1) * chan] * slope * mask
            out[at, :] = (value * factor_one).astype(BF16)
            if not 0 <= m < rows:
                continue
            g1[m * chan : (m + 1) * chan, :] = value[:, :frame_dev]
            if m % 4 == 3:
                part = g1[(m - 3) * chan : (m + 1) * chan, :]
                high = lax.reduce_precision(part, 8, 7)
                low = (part - high).astype(BF16)
                taps_in = x3[:, :frame_dev]
                products = dot(high.astype(BF16), taps_in, ((1,), (1,))) + dot(low, taps_in, ((1,), (1,)))
                for k in range(4):
                    table = table + pltpu.roll(products[k * chan : (k + 1) * chan], 128 - (m + k), 1)
    tap = iota((16, 128), 0)
    lane = iota((16, 128), 1)
    i = (tap * 11) >> 5
    select = ((lane == BAND * (tap - 3 * i) + i) & (tap < 9)) | ((lane == 3 * BAND) & (tap == 9))
    rows10 = dot(select.astype(F32), table, ((1,), (1,)), EXACT)
    share = received.shape[0] - 2
    mine = received[1 : share + 1]
    single = to_column(received[share + 1 :], share)
    factor_l = params[2:3] * stats_two[chan : chan + 1, :chan]
    mine = mine[:, :chan] - (bias_sum * single + gain_sum * mine[:, chan:]) / total
    mine = factor_l * mine
    lower = -(-share // 2)
    mine = jnp.concatenate([mine] + [jnp.zeros((2 * lower - share, chan), F32)] * (share % 2), axis=0)
    mine = jnp.concatenate([mine[:lower], mine[lower:]], axis=1)
    if lower < 9:
        mine = jnp.concatenate([mine, jnp.zeros((9 - lower, 128), F32)], axis=0)
    sums = jnp.concatenate([rows10[0:5], rows10[5:10]], axis=1)
    block = jnp.concatenate([sums, mine], axis=0)
    for d in range(devices):
        payload[14 * d : 14 * (d + 1), :] = block
    wait_all(stores)


def transposed(low, w1, x3, stats, masks, ws_hbm, first, normed, ws, pre_one, sem):
    load = pltpu.make_async_copy(ws_hbm, ws, sem)
    load.start()
    chan = low.shape[0] // (MEL_ROWS + 2)
    wide = low.shape[1]
    pre_one[...] = dot(w1[2 * chan : (MEL_ROWS + 4) * chan], x3[...])
    mean = jnp.broadcast_to(stats[0:chan, 0:1], (chan, wide))
    inv = jnp.broadcast_to(stats[0:chan, 1:2], (chan, wide))
    for q in range(MEL_ROWS + 2):
        at = slice(q * chan, (q + 1) * chan)
        mask = masks[0:1] * row_valid(q - 1, MEL_ROWS)
        normed[at, :] = ((pre_one[at, :] - mean) * inv * mask).astype(BF16)
    load.wait()
    first[...] = dot(ws[...], low[...])


def finish(recv, features, stats, k1t, first, normed, ws, params, masks,
           spec_hbm, kernel_one_hbm, kernel_two_hbm, gain_hbm, bias_hbm,
           table, spec_grad, kernel_one, kernel_two, gain_out, bias_out, sems):
    chan = params.shape[1]
    rows = MEL_ROWS
    wide = normed.shape[1]
    frame_dev = wide - RIM
    usable, behind, ahead = (masks[n : n + 1] for n in range(3))
    total = masks[3:4, 0:1]
    gain = params[0:1]
    count = recv.shape[0] // 14
    share = -(-9 * chan // count)
    lower = -(-share // 2)
    left = [recv[pl.ds(5 + p, count, stride=14), :] for p in range(lower)]
    whole = jnp.concatenate([v[:, :chan] for v in left] + [v[:, chan:] for v in left], axis=0)
    for t in range(9):
        kernel_two[t] = whole[t * chan : (t + 1) * chan].T
    stores = [pltpu.make_async_copy(kernel_two, kernel_two_hbm, sems.at[3])]
    stores[0].start()
    sums = summed_blocks(recv, count)[0:5]
    ten = jnp.concatenate([sums[:, :chan], sums[:, chan:]], axis=0)
    bias_sum = ten[9:10]
    mean_l, inv_l = stats[chan : chan + 1, :chan], stats[chan + 8 : chan + 9, :chan]
    ten = ten - features[1:2, 0:1] * bias_sum
    k = k1t[0:9]
    gain_sum = inv_l * (jnp.sum(k * ten[0:9], axis=0, keepdims=True) - mean_l * bias_sum)
    gain_out[...] = gain_sum
    bias_out[...] = bias_sum
    for n, (source, target) in enumerate(((gain_out, gain_hbm), (bias_out, bias_hbm))):
        stores.append(pltpu.make_async_copy(source, target, sems.at[n]))
        stores[-1].start()
    factor_l = gain * inv_l
    scale = factor_l * gain_sum / total
    scale = jnp.concatenate([scale, scale], axis=1)
    scale = jnp.concatenate([scale] * ((rows + 2) // 2), axis=1)
    taps = first[...] - dot((ws[...].astype(F32) * scale).astype(BF16), normed[...])
    for part in range(wide // 128):
        table[part] = taps[:, 128 * part : 128 * (part + 1)]
    moved = [
        jnp.concatenate([table[part, pl.ds(b, rows, stride=8), :] for part in range(wide // 128)], axis=1)
        for b in range(3)
    ]
    constant = jnp.sum(k * (factor_l * bias_sum / total), axis=1, keepdims=True)
    for a in range(3):
        row = iota((rows, 1), 0) + (a - 1) + lax.axis_index("mel") * rows
        valid = ((row >= 0) & (row < lax.axis_size("mel") * rows)).astype(F32) * usable
        for b in range(3):
            t = 3 * (2 - a) + 2 - b
            moved[b] = moved[b] - constant[t : t + 1] * valid
    result = pltpu.roll(moved[0], 1, 1) * behind + moved[1] + pltpu.roll(moved[2], wide - 1, 1) * ahead
    spec_grad[0] = (result * usable)[:, :frame_dev]
    stores.append(pltpu.make_async_copy(spec_grad, spec_hbm, sems.at[2]))
    stores[-1].start()
    row = features[0:1, :]
    lane = iota((1, 128), 1)
    gram = jnp.concatenate(
        [jnp.where(lane < 9, pltpu.roll(row, 128 - 9 * t, 1) if t else row, 0.0) for t in range(9)]
        + [jnp.zeros((7, 128), F32)],
        axis=0,
    )
    single = to_column(row, 16, 81)[0:9]
    k_rows = jnp.concatenate([k1t[...], jnp.zeros((112, chan), F32)], axis=0)
    normed_taps = inv_l * (dot(gram, k_rows, precision=EXACT)[0:9] - single * mean_l)
    grad_taps = factor_l * (ten[0:9] - (bias_sum * single + gain_sum * normed_taps) / total)
    for i in range(3):
        kernel_one[i] = grad_taps[3 * i : 3 * i + 3]
    stores.append(pltpu.make_async_copy(kernel_one, kernel_one_hbm, sems.at[4]))
    stores[-1].start()
    for store in stores:
        store.wait()


def run(kernel, outs, scratch, *args, hbm=0, apart=(), flops=10**8, size=4 * 10**6):
    vmem = pl.BlockSpec(memory_space=pltpu.VMEM)
    devices = lax.axis_size("mel") * lax.axis_size("tm")
    specs = []
    args = list(args)
    for n, a in enumerate(args):
        if hbm and n >= len(args) - hbm:
            specs.append(pl.BlockSpec(memory_space=pltpu.HBM))
            args[n] = pltpu.with_memory_space_constraint(a, pltpu.HBM)
        else:
            specs.append(vmem)
            args[n] = pltpu.with_memory_space_constraint(a, pltpu.VMEM)
    return pl.pallas_call(
        kernel,
        out_shape=outs,
        in_specs=specs,
        out_specs=[pl.BlockSpec(memory_space=pltpu.HBM) if n in apart else vmem for n in range(len(outs))],
        scratch_shapes=scratch,
        compiler_params=pltpu.CompilerParams(vmem_limit_bytes=(29 + devices // 32) * 2**20),
        cost_estimate=pl.CostEstimate(flops=flops, bytes_accessed=size, transcendentals=0),
    )(*args)


def shape(dims, dtype=F32):
    return jax.ShapeDtypeStruct(dims, dtype)


def kept(dims, dtype=F32):
    return pltpu.VMEM(dims, dtype)


def far(dims, dtype=F32):
    return pltpu.HBM(dims, dtype)


def exchange(blocks, axes=AXES):
    return lax.all_to_all(blocks, axes, 0, 0, tiled=True)


def exchange_rows(rows, axes=AXES):
    return exchange(rows[:, None, :], axes)[:, 0, :]


def shards(spectrum, clip_bounds, kernel_one, gain_one, bias_one, kernel_two, gain_two, bias_two, pooled_grad):
    _, rows, frame_dev = spectrum.shape
    chan = kernel_two.shape[0]
    n_mel, n_tm = lax.axis_size("mel"), lax.axis_size("tm")
    devices = n_mel * n_tm
    half = frame_dev // 2
    wide = frame_dev + RIM
    mels = n_mel * rows

    packed, own, spec, masks = run(
        pack,
        [
            kept((devices, FIRST, 128), BF16),
            kept(pooled_grad.shape, BF16),
            kept(spectrum.shape, BF16),
            kept((8, wide)),
        ],
        [
            pltpu.SMEM(clip_bounds.shape, jnp.int32),
            pltpu.VMEM((2 * chan, half), F32),
            pltpu.VMEM((devices * FIRST, 128), F32),
            pltpu.SemaphoreType.DMA((3,)),
        ],
        spectrum,
        pooled_grad,
        clip_bounds,
        hbm=3,
    )
    recv = exchange(packed)
    ext = rows + 6
    span = 4 * 3 * chan
    wf, wb, w1, ws, pairs, singles, k1t, params, all_masks, edge_masks, twice, own_rows = run(
        weights,
        [
            kept((2 * chan, span), BF16),
            kept((2 * chan, span), BF16),
            kept((ext * chan, 128), BF16),
            far((rows * 8, (rows + 2) * chan), BF16),
            kept((chan, 128)),
            kept((chan, 128)),
            kept((16, chan)),
            kept((8, chan)),
            kept((8, n_tm * frame_dev)),
            kept((n_tm * 8, 128)),
            kept((128, 128)),
            kept((chan * rows // 2, half), BF16),
        ],
        [
            pltpu.VMEM((9, chan, chan), BF16),
            pltpu.VMEM((3, 3, chan), BF16),
            pltpu.VMEM((4, 1, chan), F32),
            pltpu.SMEM(clip_bounds.shape, jnp.int32),
            pltpu.VMEM((rows * 8, (rows + 2) * chan), BF16),
            pltpu.VMEM((chan * rows // 2, half), F32),
            pltpu.SemaphoreType.DMA((8,)),
        ],
        own,
        clip_bounds,
        jnp.transpose(kernel_two, (2, 3, 0, 1)).reshape(9, chan, chan),
        jnp.transpose(kernel_one, (1, 2, 0)),
        gain_one[None],
        bias_one[None],
        gain_two[None],
        bias_two[None],
        hbm=7,
        apart=(3,),
    )
    pre_two, payload, act, x3, stats_one, features = run(
        forward_one,
        [
            kept(((rows + 4) * chan, wide)),
            kept((devices, SECOND, 128), BF16),
            kept((ext * 3 * chan, wide), BF16),
            kept((128, wide), BF16),
            kept((2 * chan + 16, 128)),
            kept((8, 128)),
        ],
        [
            pltpu.VMEM((ext * chan, wide), F32),
            pltpu.VMEM((devices * FIRST, 128), F32),
            pltpu.VMEM((n_tm * 8, 128), F32),
            pltpu.VMEM((mels + 8, RIM), F32),
            pltpu.VMEM((devices * SECOND, 128), F32),
        ],
        recv,
        spec,
        pairs,
        singles,
        twice,
        w1,
        wf,
        params,
        masks,
        all_masks,
        edge_masks,
    )
    recv = exchange(payload)
    grad, payload, stats_two = run(
        backward_scaled,
        [
            kept(((rows + 4) * chan, wide)),
            kept((devices * sum_rows(devices, 9 * chan), 128)),
            kept((chan + 8, 128)),
        ],
        [
            pltpu.VMEM(((rows // 2 + 2) * chan, RIM), F32),
            pltpu.VMEM((3 * chan + 16, rows * frame_dev), BF16),
            pltpu.VMEM((devices * SECOND, 128), F32),
            pltpu.VMEM((2 * chan, half), F32),
        ],
        recv,
        pre_two,
        act,
        own_rows,
        params,
        masks,
    )
    recv = exchange_rows(payload)
    low, payload, gain_two_grad, bias_two_grad, pre_two = run(
        backward,
        [
            kept(((rows + 2) * chan, wide), BF16),
            kept((devices * 14, 128)),
            shape((1, chan)),
            shape((1, chan)),
            far((rows // 2, 2 * chan, frame_dev)),
        ],
        [
            pltpu.VMEM(((rows + 4) * 3 * chan, wide), BF16),
            pltpu.VMEM(((rows + 2) * chan, wide), F32),
            pltpu.VMEM((rows * chan, frame_dev), F32),
            pltpu.SemaphoreType.DMA((rows // 2,)),
        ],
        recv,
        pre_two,
        grad,
        stats_two,
        w1,
        x3,
        stats_one,
        params,
        masks,
        wb,
        apart=(4,),
    )
    recv = exchange_rows(payload)
    (pooled,) = run(
        pool,
        [shape((1, chan, rows // 2, half), BF16)],
        [
            pltpu.VMEM((rows // 2 * chan, 128), F32),
            pltpu.VMEM((rows // 2, 2 * chan, frame_dev), F32),
            pltpu.SemaphoreType.DMA((rows // 2,)),
        ],
        payload,
        stats_two,
        masks,
        pre_two,
        hbm=1,
    )
    first, normed, ws = run(
        transposed,
        [
            kept((rows * 8, wide)),
            kept(((rows + 2) * chan, wide), BF16),
            kept((rows * 8, (rows + 2) * chan), BF16),
        ],
        [pltpu.VMEM(((rows + 2) * chan, wide), F32), pltpu.SemaphoreType.DMA],
        low,
        w1,
        x3,
        stats_one,
        masks,
        ws,
        hbm=1,
    )
    spec_grad, kernel_one_grad, kernel_two_grad, gain_one_grad, bias_one_grad = run(
        finish,
        [
            shape((1, rows, frame_dev)),
            shape((3, 3, chan)),
            shape((9, chan, chan)),
            shape((1, chan)),
            shape((1, chan)),
        ],
        [
            pltpu.VMEM((3, rows * 8, 128), F32),
            pltpu.VMEM((1, rows, frame_dev), F32),
            pltpu.VMEM((3, 3, chan), F32),
            pltpu.VMEM((9, chan, chan), F32),
            pltpu.VMEM((1, chan), F32),
            pltpu.VMEM((1, chan), F32),
            pltpu.SemaphoreType.DMA((5,)),
        ],
        recv,
        features,
        stats_one,
        k1t,
        first,
        normed,
        ws,
        params,
        masks,
        apart=range(5),
    )
    kernel_two_grad = jnp.transpose(kernel_two_grad.reshape(3, 3, chan, chan), (2, 3, 0, 1))
    return (
        pooled,
        spec_grad,
        jnp.transpose(kernel_one_grad, (2, 0, 1)),
        gain_one_grad[0],
        bias_one_grad[0],
        kernel_two_grad,
        gain_two_grad[0],
        bias_two_grad[0],
    )


def solution(mesh):
    return jax.shard_map(
        shards,
        mesh=mesh,
        in_specs=(
            P(None, "mel", "tm"),
            P(),
            P(),
            P(),
            P(),
            P(),
            P(),
            P(),
            P(None, None, "mel", "tm"),
        ),
        out_specs=(P(None, None, "mel", "tm"), P(None, "mel", "tm"), P(), P(), P(), P(), P(), P()),
        check_vma=False,
    )
```

```python
import math

import jax
import jax.numpy as jnp
from jax import lax
from jax.experimental import pallas as pl
from jax.experimental.pallas import tpu as pltpu
from jax.sharding import PartitionSpec as P

F32 = jnp.float32
BF16 = jnp.bfloat16
AXES = ("mel", "tm")
EXACT = lax.Precision.HIGHEST
RIM = 128
BAND = 24
MEL_ROWS = 16
FIRST = 24
SUMS, EDGES, COLUMNS = 16, 19, 23
SIDE = 96
SECOND = 8


def iota(shape, dim):
    return lax.broadcasted_iota(jnp.int32, shape, dim)


def dot(a, b, over=((1,), (0,)), precision=None):
    return lax.dot_general(a, b, (over, ((), ())), precision=precision, preferred_element_type=F32)


def to_column(lanes, count, start=0):
    shape = (count, lanes.shape[1])
    return jnp.sum(jnp.where(iota(shape, 1) == iota(shape, 0) + start, lanes, 0.0), axis=1, keepdims=True)


def to_lanes(column, start=0, width=128):
    shape = (column.shape[0], width)
    return jnp.sum(jnp.where(iota(shape, 1) == iota(shape, 0) + start, column, 0.0), axis=0, keepdims=True)


def halves(v):
    total = v[:, :128]
    for n in range(128, v.shape[1], 128):
        total = total + v[:, n : n + 128]
    return total


def frame_masks(bounds, frames):
    last = bounds.shape[1] - 1

    def living(f):
        return (f >= 0) & (f < bounds[0, last])

    def paired(f):
        both = living(f) & living(f + 1)
        for k in range(1, last):
            both = both & (f + 1 != bounds[0, k])
        return both

    return tuple(m.astype(F32) for m in (living(frames), paired(frames - 1), paired(frames)))


def row_valid(row, rows):
    mel = lax.axis_index("mel") * rows + row
    return ((mel >= 0) & (mel < lax.axis_size("mel") * rows)).astype(F32)


def start_all(*pairs, sems):
    copies = [pltpu.make_async_copy(src, dst, sems.at[n]) for n, (src, dst) in enumerate(pairs)]
    for copy in copies:
        copy.start()
    return copies


def wait_all(copies):
    for copy in copies:
        copy.wait()


def shifted_frames(value, behind, ahead):
    wide = value.shape[1]
    return pltpu.roll(value, 1, 1) * behind, pltpu.roll(value, wide - 1, 1) * ahead


def three_parts(v):
    high = lax.reduce_precision(v, 8, 7)
    mid = lax.reduce_precision(v - high, 8, 7)
    return high, mid, v - high - mid


def share_of(devices, chan):
    return -(-chan // devices)


def pack(spec_hbm, grad_hbm, bounds_hbm, out, own, spec, masks, bounds, edges, rows_out, sems):
    copies = start_all((bounds_hbm, bounds), (spec_hbm, spec), (grad_hbm, own), sems=sems)
    copies[0].wait()
    wide = masks.shape[1]
    frame_dev = wide - RIM
    devices = out.shape[0]
    rows = MEL_ROWS
    lane = iota((1, wide), 1)
    frames = lax.axis_index("tm") * frame_dev + jnp.where(lane < frame_dev + RIM // 2, lane, lane - wide)
    last = bounds.shape[1] - 1
    pixels = (bounds[0, last] * (lax.axis_size("mel") * rows)).astype(F32)
    found = frame_masks(bounds, frames)
    masks[...] = jnp.concatenate(
        list(found) + [jnp.full((1, wide), 1.0) * pixels, jnp.zeros((4, wide), F32)], axis=0
    )
    usable, behind, ahead = (m[:, :frame_dev] for m in found)
    copies[1].wait()
    x = spec[0].astype(F32) * usable
    lane = iota((1, frame_dev), 1)
    row = iota((rows, 1), 0)
    inner = jnp.where((lane > 0) & (lane < frame_dev - 1), usable, 0.0)
    number = (rows - 2) * jnp.sum(inner, axis=1, keepdims=True)
    inner = inner * ((row > 0) & (row < rows - 1)).astype(F32)
    centre = jnp.sum(jnp.sum(x, axis=0, keepdims=True), axis=1, keepdims=True)
    centre = centre / (rows * jnp.maximum(jnp.sum(usable, axis=1, keepdims=True), 1.0))
    centre = lax.reduce_precision(centre, 8, 7)
    shifted = [pltpu.roll(x, 1, 1) * behind, x, pltpu.roll(x, frame_dev - 1, 1) * ahead]
    taps = [pltpu.roll(v, (1 - i) % rows, 0) if i != 1 else v for i in range(3) for v in shifted]
    features = feature_rows(centre, (taps, inner))
    lane = iota((1, 128), 1)
    features = jnp.where(lane == 90, centre, jnp.where(lane == 91, number, features))
    pick = iota((8, frame_dev), 0)
    column = jnp.where(pick < 4, pick, frame_dev - 8 + pick)
    strip = dot((iota((8, frame_dev), 1) == column).astype(BF16), x.astype(BF16), ((1,), (1,)))
    lane = iota((8, 128), 1)
    repeat = (iota((rows, 128), 1) % rows == iota((rows, 128), 0)).astype(BF16)
    strip = jnp.where(lane // rows == iota((8, 128), 0), dot(strip.astype(BF16), repeat), 0.0)
    strip = jnp.sum(strip, axis=0, keepdims=True)

    def put(n, value):
        rows_out[pl.ds(n, devices, stride=FIRST), :] = jnp.broadcast_to(value, (devices, 128))

    near = jnp.concatenate([x[0:4], x[rows - 4 :]], axis=0)
    for n in range(8):
        put(n, near[n : n + 1, :128])
        put(8 + n, near[n : n + 1, 128:])
    put(COLUMNS, strip)
    copies[2].wait()
    _, chan, many, half = own.shape
    share = share_of(devices, chan)
    holders = chan // share
    g = own[0].astype(F32)
    edges[0:chan] = g[:, 0, :]
    edges[chan:] = g[:, many - 1, :]

    def spread_out(v):
        if holders < devices:
            v = jnp.concatenate([v, jnp.zeros((devices - holders, 128), F32)], axis=0)
        return v

    for n in range(share):
        put(EDGES + n, spread_out(edges[n * holders : (n + 1) * holders, :]))
        put(EDGES + share + n, spread_out(edges[chan + n * holders : chan + (n + 1) * holders, :]))
    for n in range(2 * share, COLUMNS - EDGES):
        put(EDGES + n, jnp.zeros((1, 128), F32))
    end = iota((8, half), 0)
    at = iota((8, half), 1)
    ends = ((end == 0) & (at == 0)) | ((end == 1) & (at == half - 1))
    columns = dot(ends.astype(BF16), g.reshape(chan * many, half).astype(BF16), ((1,), (1,)))
    group = 128 // many
    source = iota((128, 128), 0)
    lane = iota((group, 128), 1)
    mine = lane // many == iota((group, 128), 0)
    parts = three_parts(features)
    for n in range(2):
        side = jnp.zeros((holders, 128), F32)
        for m in range(share):
            move = (iota((128, 128), 1) == SIDE + many * m + source % many).astype(BF16)
            first = m * holders * many // 128
            block = [columns[n : n + 1, 128 * q : 128 * (q + 1)] for q in range(first, first + holders * many // 128)]
            block = jnp.concatenate([jnp.where(mine, v, 0.0) for v in block], axis=0)
            side = side + dot(block.astype(BF16), move)
        put(SUMS + n, spread_out(side) + parts[n])
    put(SUMS + 2, parts[2])
    out[...] = rows_out[...].reshape(out.shape).astype(BF16)


def weights(own, bounds_hbm, k2_hbm, k1_hbm, gain_one_hbm, bias_one_hbm, gain_two_hbm, bias_two_hbm,
            wf, wb, w1, ws_hbm, pairs, singles, k1t, params, all_masks, edge_masks, twice, own_rows,
            k2, k1, vectors, bounds, ws, temp, sems):
    loads = start_all(
        (bounds_hbm, bounds),
        (k2_hbm, k2),
        (k1_hbm, k1),
        (gain_one_hbm, vectors.at[0]),
        (bias_one_hbm, vectors.at[1]),
        (gain_two_hbm, vectors.at[2]),
        (bias_two_hbm, vectors.at[3]),
        sems=sems,
    )
    _, many, count, half = own.shape
    temp[...] = own[0].astype(F32).reshape(many * count, half)
    for r in range(count):
        own_rows[r * many : (r + 1) * many] = temp[pl.ds(r, many, stride=count), :].astype(BF16)
    wait_all(loads)
    chan = k2.shape[1]
    span = wf.shape[1]
    taps = [k2[t].astype(F32) for t in range(9)]
    rest = jnp.zeros((chan, span - 9 * chan), F32)
    forward = jnp.concatenate(taps + [rest], axis=1)
    backward = jnp.concatenate([taps[8 - t].T for t in range(9)] + [rest], axis=1)
    for r in range(wb.shape[0] // chan):
        at = slice(r * chan, (r + 1) * chan)
        wb[at] = (pltpu.roll(backward, 3 * chan * r, 1) if r else backward).astype(BF16)
    full = jnp.concatenate([k1[n].astype(F32) for n in range(3)] + [jnp.zeros((7, chan), F32)], axis=0)
    low = [
        jnp.concatenate([full[3 * (2 - a) + 2 - b : 3 * (2 - a) + 3 - b] for a in range(3)], axis=1)
        for b in range(3)
    ]
    base = jnp.concatenate(low + [jnp.zeros((5, 3 * chan), F32)], axis=0)
    base = jnp.concatenate([base, jnp.zeros((8, ws.shape[1] - 3 * chan), F32)], axis=1)
    for m in range(ws.shape[0] // 8):
        ws[8 * m : 8 * m + 8] = (pltpu.roll(base, chan * m, 1) if m else base).astype(BF16)
    store_ws = pltpu.make_async_copy(ws, ws_hbm, sems.at[7])
    store_ws.start()
    frames = all_masks.shape[1]
    frame_dev = frames // lax.axis_size("tm")
    all_masks[...] = jnp.concatenate(
        list(frame_masks(bounds, iota((1, frames), 1))) + [jnp.zeros((5, frames), F32)], axis=0
    )
    q = iota(edge_masks.shape, 0)
    lane = iota(edge_masks.shape, 1)
    k = q % 8
    frames = (q // 8) * frame_dev + jnp.where(k < 4, k, k + frame_dev - 8)
    living, behind, ahead = frame_masks(bounds, frames)
    living = jnp.where((k == 0) | (k == 7), living, 0.0)
    edge_masks[...] = jnp.where(lane == 0, living, jnp.where(lane == 1, behind, jnp.where(lane == 2, ahead, 0.0)))
    params[...] = jnp.concatenate(
        [vectors[n] for n in range(4)] + [jnp.zeros((4, chan), F32)], axis=0
    )
    tap = iota((16, 128), 0)
    lane = iota((16, 128), 1)
    i = (tap * 11) >> 5
    ninth = (lane * 57) >> 9
    to_band = (lane == BAND * (tap - 3 * i) + i) & (tap < 9)
    to_left = (ninth == tap) & (tap < 9)
    to_right = (lane - 9 * ninth == tap) & (lane < 81)
    to_single = (lane == 81 + tap) & (tap < 9)
    source = iota((128, 128), 0) - 81
    lane = iota((128, 128), 1)
    ninth = (lane * 57) >> 9
    inside = (source >= 0) & (source < 9) & (lane < 81)
    twice[...] = jnp.where(inside, (source == ninth).astype(F32) + (source == lane - 9 * ninth).astype(F32), 0.0)
    for r in range(wf.shape[0] // chan):
        at = slice(r * chan, (r + 1) * chan)
        wf[at] = (pltpu.roll(forward, 3 * chan * r, 1) if r else forward).astype(BF16)
    k1t[...] = full
    k = full.astype(BF16)
    lanes = [dot(k, select.astype(BF16), ((0,), (0,))) for select in (to_band, to_left, to_right, to_single)]
    pairs[...] = lanes[1] * lanes[2]
    singles[...] = lanes[3]
    for m in range(w1.shape[0] // chan):
        w1[m * chan : (m + 1) * chan] = (pltpu.roll(lanes[0], m, 1) if m else lanes[0]).astype(BF16)
    store_ws.wait()


def feature_rows(centre, *parts):
    def folded(v):
        return jnp.sum(halves(v), axis=0, keepdims=True)

    rows = [jnp.zeros((1, 128), F32)] * 96
    for taps, weight in parts:
        z = [tap - centre for tap in taps]
        for s in range(9):
            left = z[s] * weight
            rows[81 + s] = rows[81 + s] + folded(left)
            for t in range(s, 9):
                rows[9 * s + t] = rows[9 * t + s] = rows[9 * s + t] + folded(left * z[t])
    return to_lanes(jnp.sum(jnp.concatenate(rows, axis=0), axis=1, keepdims=True))


def summed_blocks(ref, devices):
    block = ref.shape[0] // devices
    period = 8 // math.gcd(block, 8)
    step = period * block
    total = ref[0:step, :]
    for at in range(step, ref.shape[0], step):
        total = total + ref[at : at + step, :]
    result = total[0:block]
    for n in range(1, period):
        result = result + total[n * block : (n + 1) * block]
    return result


def moved_rows(v, step):
    if step == 0:
        return v
    count = v.shape[0]
    if abs(step) >= count:
        return jnp.zeros_like(v)
    zero = jnp.zeros((abs(step), v.shape[1]), v.dtype)
    if step > 0:
        return jnp.concatenate([zero, v[: count - step]], axis=0)
    return jnp.concatenate([v[-step:], zero], axis=0)


def silu_halves(h):
    t = jnp.tanh(h)
    one = 1.0 + t
    return h * one, one * (1.0 + h * (1.0 - t))


def forward_one(recv, spec, pairs, singles, twice, w1, wf, params, masks, all_masks, edge_masks,
                pre_two, payload, act, x3, stats, features_out, pre_one, got, strips, halo, rows_out):
    devices = recv.shape[0]
    n_mel, count = lax.axis_size("mel"), lax.axis_size("tm")
    rows = MEL_ROWS
    mels = n_mel * rows
    wide = masks.shape[1]
    frame_dev = wide - RIM
    chan = params.shape[1]
    me_m, me_t = lax.axis_index("mel"), lax.axis_index("tm")
    usable, behind, ahead = (masks[n : n + 1] for n in range(3))
    total = masks[3:4, 0:1]
    got[...] = recv[...].astype(F32).reshape(devices * FIRST, 128)

    def every(n):
        return got[pl.ds(n, devices, stride=FIRST), :]

    lane = iota((count, 128), 1)
    bands = [got[pl.ds(FIRST * k * count + COLUMNS, count, stride=FIRST), :] for k in range(n_mel)]
    for c in range(8):
        column = jnp.zeros((count, 128), F32)
        for k, band in enumerate(bands):
            part = jnp.where(lane // rows == c, band, 0.0)
            column = column + (pltpu.roll(part, rows * (k - c) % 128, 1) if k != c else part)
        strips[pl.ds(c, count, stride=8), :] = column
    at = pl.multiple_of(FIRST * (jnp.maximum(me_m - 1, 0) * count + me_t), 8)
    above = got[pl.ds(at, 16), :] * (me_m > 0).astype(F32)
    at = pl.multiple_of(FIRST * (jnp.minimum(me_m + 1, n_mel - 1) * count + me_t), 8)
    below = got[pl.ds(at, 16), :] * (me_m < n_mel - 1).astype(F32)
    above = jnp.concatenate([above[4:8], above[12:16]], axis=1)
    below = jnp.concatenate([below[0:4], below[8:12]], axis=1)
    own = spec[0].astype(F32) * usable[:, :frame_dev]
    at = pl.multiple_of(8 * jnp.minimum(me_t + 1, count - 1), 8)
    after = strips[pl.ds(at, 8), :][:, :mels] * (me_t + 1 < count).astype(F32)
    at = pl.multiple_of(8 * jnp.maximum(me_t - 1, 0), 8)
    before = strips[pl.ds(at, 8), :][:, :mels] * (me_t > 0).astype(F32)
    sides = jnp.concatenate([after[0:4], before[4:8], jnp.zeros((8, mels), F32)], axis=0).astype(BF16)
    side = iota((16, RIM), 0)
    place = iota((16, RIM), 1) == jnp.where(side < 4, side, jnp.where(side < 8, side + RIM - 8, -1))
    halo[0:8] = jnp.zeros((8, RIM), F32)
    halo[mels : mels + 8] = jnp.zeros((8, RIM), F32)
    halo[4 : mels + 4] = dot(sides, place.astype(BF16), ((0,), (0,)))
    rim = halo[pl.ds(pl.multiple_of(me_m * rows, 8), BAND), :]
    near = jnp.concatenate([jnp.concatenate([above, own, below], axis=0), rim], axis=1)
    x3[...] = jnp.concatenate(
        [
            pltpu.roll(near, 1, 1) * behind,
            near,
            pltpu.roll(near, wide - 1, 1) * ahead,
            jnp.broadcast_to(usable, (BAND, wide)),
            jnp.zeros((128 - 4 * BAND, wide), F32),
        ],
        axis=0,
    ).astype(BF16)
    pre_one[...] = dot(w1[...], x3[...])
    lane = iota((1, 128), 1)
    parts = jnp.where(lane < 92, every(SUMS) + every(SUMS + 1) + every(SUMS + 2), 0.0)
    centres, numbers = parts[:, 90:91], parts[:, 91:92]
    centre = jnp.sum(centres * numbers, axis=0, keepdims=True)
    centre = centre / jnp.maximum(jnp.sum(numbers, axis=0, keepdims=True), 1.0)
    delta = centres - centre
    features = jnp.sum(parts + delta * numbers * jnp.where(lane < 81, delta, 1.0), axis=0, keepdims=True)
    moved = jnp.sum(delta * parts, axis=0, keepdims=True)
    moved = dot(jnp.broadcast_to(moved, (8, 128)), twice[...], precision=EXACT)[0:1]
    features = features + moved
    tiles = []
    for k in range(n_mel):
        lanes = []
        for d in range(count):
            at = FIRST * (k * count + d)
            lanes += [got[at : at + 8, :], got[at + 8 : at + 16, :]]
        tiles.append(jnp.concatenate(lanes, axis=1))
    zero = jnp.zeros((1, tiles[0].shape[1]), F32)
    before_row, this_row, next_row = [], [], []
    for k, tile in enumerate(tiles):
        before_row += [tiles[k - 1][7:8] if k else zero, tile[6:7]]
        this_row += [tile[0:1], tile[7:8]]
        next_row += [tile[1:2], tiles[k + 1][0:1] if k + 1 < n_mel else zero]
    f_usable, f_behind, f_ahead = (all_masks[n : n + 1] for n in range(3))
    taps = []
    for group in (before_row, this_row, next_row):
        v = jnp.concatenate(group, axis=0)
        taps += [pltpu.roll(v, 1, 1) * f_behind, v, pltpu.roll(v, v.shape[1] - 1, 1) * f_ahead]
    borders = (taps, f_usable)
    edge = strips[...]
    q_usable, q_behind, q_ahead = (edge_masks[:, n : n + 1] for n in range(3))
    lane = iota((count * 8, 128), 1)
    inside = (lane < mels) & (lane % rows != 0) & (lane % rows != rows - 1)
    shifted = [
        pltpu.roll(edge, 1, 0) * q_behind,
        edge,
        pltpu.roll(edge, count * 8 - 1, 0) * q_ahead,
    ]
    taps = [pltpu.roll(v, (1 - i) % 128, 1) if i != 1 else v for i in range(3) for v in shifted]
    features = features + feature_rows(centre, borders, (taps, jnp.where(inside, q_usable, 0.0)))
    features = jnp.where(iota((1, 128), 1) < 90, features, 0.0)
    features_out[...] = jnp.concatenate(
        [features, jnp.broadcast_to(centre, (1, 128)), jnp.zeros((6, 128), F32)], axis=0
    )
    near_mean = jnp.sum(singles[...] * features, axis=1, keepdims=True) / total
    square = jnp.sum(pairs[...] * features, axis=1, keepdims=True) / total
    inv = lax.rsqrt(square - near_mean * near_mean + 1e-05)
    mean = near_mean + centre * jnp.sum(singles[...], axis=1, keepdims=True)
    lane = iota((chan, 128), 1)
    stats[0:chan] = jnp.where(lane == 0, mean, jnp.where(lane == 1, inv, 0.0))
    stats[chan : chan + 8] = jnp.broadcast_to(to_lanes(near_mean), (8, 128))
    stats[chan + 8 : chan + 16] = jnp.broadcast_to(to_lanes(inv), (8, 128))
    scale = 0.5 * to_column(params[0:1], chan) * inv
    shift = 0.5 * to_column(params[1:2], chan) - mean * scale
    stats[chan + 16 :] = jnp.where(lane == 0, scale, jnp.where(lane == 1, shift, 0.0))
    scale = jnp.broadcast_to(scale, (chan, wide))
    shift = jnp.broadcast_to(shift, (chan, wide))
    ext = w1.shape[0] // chan
    block, taps = wf.shape
    first = jnp.zeros((chan, 128), F32)
    second = jnp.zeros((chan, 128), F32)
    own_mask = usable[:, :frame_dev]
    low_masks = [m.astype(BF16) for m in (usable, behind, ahead)]
    for r in range(ext):
        value, _ = silu_halves(pre_one[r * chan : (r + 1) * chan, :] * scale + shift)
        if not 0 <= r - 3 < rows:
            value = value * row_valid(r - 3, rows)
        base = r * 3 * chan
        low = value.astype(BF16) * low_masks[0]
        act[base : base + chan, :], act[base + 2 * chan : base + 3 * chan, :] = shifted_frames(low, *low_masks[1:])
        act[base + chan : base + 2 * chan, :] = low
        if r < 3 or r % 2 == 0:
            continue
        g = (r - 3) // 2
        result = dot(wf[...], act[g * 3 * block : g * 3 * block + taps, :])
        pre_two[g * block : (g + 1) * block] = result
        for q in range(2):
            if 2 <= 2 * g + q < rows + 2:
                p = result[q * chan : (q + 1) * chan, :frame_dev]
                masked = p * own_mask
                first = first + halves(masked)
                second = second + halves(masked * p)
    share = share_of(devices, chan)

    def put(n, value):
        rows_out[pl.ds(n, devices, stride=SECOND), :] = jnp.broadcast_to(value, (devices, 128))

    for n in range(share):
        put(3 + n, moved_rows(every(EDGES + share + n), count))
        put(3 + share + n, moved_rows(every(EDGES + n), -count))
    for n in range(3 + 2 * share, SECOND - 1):
        put(n, jnp.zeros((1, 128), F32))
    lane = iota((devices, 128), 1)
    tm = iota((devices, 128), 0) % count
    lefts = jnp.where(lane >= SIDE, every(SUMS), 0.0)
    rights = jnp.where(lane >= SIDE, every(SUMS + 1), 0.0)
    beside = jnp.zeros((devices, 128), F32)
    for n, step in enumerate((0, count, -count)):
        one = jnp.where(tm > 0, moved_rows(rights, step + 1), 0.0)
        two = jnp.where(tm < count - 1, moved_rows(lefts, step - 1), 0.0)
        beside = beside + pltpu.roll(one, (32 * n - SIDE) % 128, 1) + pltpu.roll(two, (32 * n + 16 - SIDE) % 128, 1)
    put(SECOND - 1, beside)
    first = jnp.sum(first, axis=1, keepdims=True)
    second = jnp.sum(second, axis=1, keepdims=True)
    for n, part in enumerate(three_parts(to_lanes(first) + to_lanes(second, chan))):
        put(n, part)
    payload[...] = rows_out[...].reshape(payload.shape).astype(BF16)


def sum_rows(devices, taps):
    return -(-taps // devices) + 2


def backward_scaled(recv, pre_two, act, own_rows, params, masks,
                    grad, payload, stats, sides, right, got, beyond):
    devices = recv.shape[0]
    got[...] = recv[...].astype(F32).reshape(devices * SECOND, 128)
    chan = params.shape[1]
    half = own_rows.shape[1]
    lane = iota((half, 2 * half), 1)
    spread = jnp.where(lane >> 1 == iota((half, 2 * half), 0), 0.25, 0.0).astype(BF16)
    rows = MEL_ROWS
    wide = pre_two.shape[1]
    frame_dev = wide - RIM
    usable = masks[0:1]
    share = share_of(devices, chan)
    holders = chan // share

    def every(n):
        return got[pl.ds(n, devices, stride=SECOND), :]

    beside = every(SECOND - 1)[:holders]
    lane = iota((holders, RIM), 1)
    many = rows // 2
    for n in range(share):
        first = n * holders
        beyond[first : first + holders, :] = every(3 + n)[:holders]
        beyond[chan + first : chan + first + holders, :] = every(3 + share + n)[:holders]
        for r in range(many + 2):
            at = many * n + (r if r < many else 32 + many - 1 if r == many else 64)
            left, right_of = beside[:, at : at + 1], beside[:, at + 16 : at + 17]
            side = jnp.where(lane >= RIM - 2, 0.25 * left, jnp.where(lane < 2, 0.25 * right_of, 0.0))
            sides[r * chan + first : r * chan + first + holders, :] = side
    total = masks[3:4, 0:1]
    sums = jnp.sum(every(0) + every(1) + every(2), axis=0, keepdims=True)
    mean = to_column(sums, chan) / total
    inv = lax.rsqrt(to_column(sums, chan, chan) / total - mean * mean + 1e-05)
    lane = iota((chan, 128), 1)
    scale = 0.5 * to_column(params[2:3], chan) * inv
    shift = 0.5 * to_column(params[3:4], chan) - mean * scale
    columns = jnp.zeros((chan, 128), F32)
    for n, column in enumerate((mean, inv, scale, shift)):
        columns = jnp.where(lane == n, column, columns)
    stats[0:chan] = columns
    stats[chan : chan + 8] = jnp.broadcast_to(to_lanes(inv), (8, 128))
    shift = jnp.broadcast_to(shift, (chan, wide))
    scale = jnp.broadcast_to(scale, (chan, wide))
    mean = jnp.broadcast_to(mean, (chan, frame_dev))
    inv = jnp.broadcast_to(inv, (chan, frame_dev))
    first = jnp.zeros((chan, 128), F32)
    second = jnp.zeros((chan, 128), F32)
    right[3 * chan :] = jnp.ones((16, rows * frame_dev), BF16)
    table = jnp.zeros((9 * chan, 3 * chan + 16), F32)
    for q in list(range(2, rows + 2)) + [0, 1, rows + 2, rows + 3]:
        r = q // 2
        at = slice(q * chan, (q + 1) * chan)
        m = q - 2
        mask = 0.5 * usable if 0 <= m < rows else usable * (0.5 * row_valid(m, rows))
        if q % 2 == 0:
            if 1 <= r <= rows // 2:
                pooled, at_side = own_rows[(r - 1) * chan : r * chan], (r - 1) * chan
            elif r == 0:
                pooled, at_side = beyond[0:chan].astype(BF16), many * chan
            else:
                pooled, at_side = beyond[chan:].astype(BF16), (many + 1) * chan
            up = jnp.concatenate([dot(pooled, spread), sides[at_side : at_side + chan, :]], axis=1)
        pre = pre_two[at, :]
        _, slope = silu_halves(pre * scale + shift)
        g = up * slope * mask
        grad[at, :] = g
        if not 0 <= m < rows:
            continue
        g = g[:, :frame_dev]
        normed = (pre[:, :frame_dev] - mean) * inv
        first = first + halves(g * normed)
        second = second + halves(g)
        lanes = slice(m * frame_dev, (m + 1) * frame_dev)
        high = lax.reduce_precision(g, 8, 7)
        right[0:chan, lanes] = high.astype(BF16)
        right[chan : 2 * chan, lanes] = (g - high).astype(BF16)
        right[2 * chan : 3 * chan, lanes] = normed.astype(BF16)
        if m % 4 == 3:
            left = [act[(n + 2) * 3 * chan : (n + 5) * 3 * chan, :frame_dev] for n in range(m - 3, m + 1)]
            lanes = slice((m - 3) * frame_dev, (m + 1) * frame_dev)
            table = table + dot(jnp.concatenate(left, axis=1), right[:, lanes], ((1,), (1,)))
    first = jnp.sum(first, axis=1, keepdims=True)
    second = jnp.sum(second, axis=1, keepdims=True)
    totals = to_lanes(first) + to_lanes(second, chan)
    block = payload.shape[0] // devices
    payload[pl.ds(0, devices, stride=block), :] = jnp.broadcast_to(totals, (devices, 128))
    both = jnp.concatenate([table[:, :chan] + table[:, chan : 2 * chan], table[:, 2 * chan : 3 * chan]], axis=1)
    single = table[:, 3 * chan : 3 * chan + 1]
    lane = iota((devices, 128), 1)
    constants = jnp.zeros((devices, 128), F32)
    for k in range(block - 2):
        cut, ones = both[k * devices : (k + 1) * devices], single[k * devices : (k + 1) * devices]
        short = devices - cut.shape[0]
        if short:
            cut = jnp.concatenate([cut, jnp.zeros((short, 128), F32)], axis=0)
            ones = jnp.concatenate([ones, jnp.zeros((short, 1), F32)], axis=0)
        payload[pl.ds(1 + k, devices, stride=block), :] = cut
        constants = jnp.where(lane == k, ones, constants)
    payload[pl.ds(block - 1, devices, stride=block), :] = constants


def pool(after, stats, masks, pre_hbm, out, temp, pre_two, sems):
    del after
    chan, rows, half = out.shape[1:]
    frame_dev = 2 * half
    step = pre_two.shape[0] // 2
    loads = start_all(
        *((pre_hbm.at[pl.ds(n * step, step), :], pre_two.at[pl.ds(n * step, step), :]) for n in range(2)), sems=sems
    )
    to_mean = jnp.where(iota((frame_dev, half), 0) >> 1 == iota((frame_dev, half), 1), 0.25, 0.0)
    usable = masks[0:1, :frame_dev]
    scale = jnp.broadcast_to(stats[0:chan, 2:3], (chan, frame_dev))
    shift = jnp.broadcast_to(stats[0:chan, 3:4], (chan, frame_dev))
    for r in range(rows):
        if r % (rows // 2) == 0:
            loads[2 * r // rows].wait()
        at = 2 * r * chan
        both = [
            silu_halves(pre_two[at + h * chan : at + (h + 1) * chan, :frame_dev] * scale + shift)[0] * usable
            for h in range(2)
        ]
        temp[pl.ds(r, chan, stride=rows), :] = dot(both[0] + both[1], to_mean, precision=EXACT)
    out[0] = temp[...].reshape(chan, rows, half).astype(BF16)


def backward(recv, pre_two, grad, stats_two, w1, x3, stats, params, masks, wb,
             out, payload, gain_out, bias_out, pre_hbm, g3, pre_one, g1, sem):
    chan = params.shape[1]
    rows = MEL_ROWS
    wide = pre_two.shape[1]
    frame_dev = wide - RIM
    usable = masks[0:1]
    behind, ahead = (masks[n : n + 1].astype(BF16) for n in (1, 2))
    total = masks[3:4, 0:1]
    devices = payload.shape[0] // 14
    store = pltpu.make_async_copy(pre_two.at[pl.ds(2 * chan, rows * chan), :], pre_hbm, sem)
    store.start()
    pre_one[...] = dot(w1[2 * chan : (rows + 4) * chan], x3[...])

    received = summed_blocks(recv, devices)
    sums = received[0:1]
    gain_sum, bias_sum = sums[:, :chan], sums[:, chan:]
    gain_out[...] = gain_sum
    bias_out[...] = bias_sum
    mean, inv = stats_two[0:chan, 0:1], stats_two[0:chan, 1:2]
    factor = to_column(params[2:3], chan) * inv
    gain_part = factor * (to_column(sums, chan) / total * inv)
    bias_part = factor * (to_column(sums, chan, chan) / total) - mean * gain_part
    gain_part = jnp.broadcast_to(gain_part, (chan, wide))
    bias_part = jnp.broadcast_to(bias_part, (chan, wide))
    factor = jnp.broadcast_to(factor, (chan, wide))
    scale = jnp.broadcast_to(stats[chan + 16 :, 0:1], (chan, wide))
    shift = jnp.broadcast_to(stats[chan + 16 :, 1:2], (chan, wide))
    factor_one = jnp.broadcast_to(to_column(params[0:1], chan) * stats[0:chan, 1:2], (chan, wide))
    count = pre_two.shape[0] // chan
    table = jnp.zeros((chan, 128), F32)
    for q in range(count):
        at = slice(q * chan, (q + 1) * chan)
        mask = usable if 0 <= q - 2 < rows else usable * row_valid(q - 2, rows)
        low = (factor * grad[at, :] - (bias_part + pre_two[at, :] * gain_part) * mask).astype(BF16)
        base = q * 3 * chan
        g3[base : base + chan, :], g3[base + 2 * chan : base + 3 * chan, :] = shifted_frames(low, behind, ahead)
        g3[base + chan : base + 2 * chan, :] = low
        if q < 3 or q % 2 == 0:
            continue
        start = q - 3
        result = dot(wb[...], g3[start * 3 * chan : (start + 4) * 3 * chan, :])
        for n in range(2):
            m = start + n - 1
            at = slice((m + 1) * chan, (m + 2) * chan)
            _, slope = silu_halves(pre_one[at, :] * scale + shift)
            mask = 0.5 * usable if 0 <= m < rows else usable * (0.5 * row_valid(m, rows))
            value = result[n * chan : (n + 1) * chan] * slope * mask
            out[at, :] = (value * factor_one).astype(BF16)
            if not 0 <= m < rows:
                continue
            g1[m * chan : (m + 1) * chan, :] = value[:, :frame_dev]
            if m % 4 == 3:
                part = g1[(m - 3) * chan : (m + 1) * chan, :]
                high = lax.reduce_precision(part, 8, 7)
                low = (part - high).astype(BF16)
                taps_in = x3[:, :frame_dev]
                products = dot(high.astype(BF16), taps_in, ((1,), (1,))) + dot(low, taps_in, ((1,), (1,)))
                for k in range(4):
                    table = table + pltpu.roll(products[k * chan : (k + 1) * chan], 128 - (m + k), 1)
    tap = iota((16, 128), 0)
    lane = iota((16, 128), 1)
    i = (tap * 11) >> 5
    select = ((lane == BAND * (tap - 3 * i) + i) & (tap < 9)) | ((lane == 3 * BAND) & (tap == 9))
    rows10 = dot(select.astype(F32), table, ((1,), (1,)), EXACT)
    share = received.shape[0] - 2
    mine = received[1 : share + 1]
    single = to_column(received[share + 1 :], share)
    factor_l = params[2:3] * stats_two[chan : chan + 1, :chan]
    mine = mine[:, :chan] - (bias_sum * single + gain_sum * mine[:, chan:]) / total
    mine = factor_l * mine
    lower = -(-share // 2)
    mine = jnp.concatenate([mine] + [jnp.zeros((2 * lower - share, chan), F32)] * (share % 2), axis=0)
    mine = jnp.concatenate([mine[:lower], mine[lower:]], axis=1)
    if lower < 9:
        mine = jnp.concatenate([mine, jnp.zeros((9 - lower, 128), F32)], axis=0)
    sums = jnp.concatenate([rows10[0:5], rows10[5:10]], axis=1)
    block = jnp.concatenate([sums, mine], axis=0)
    for d in range(devices):
        payload[14 * d : 14 * (d + 1), :] = block
    store.wait()


def transposed(low, w1, x3, stats, masks, ws_hbm, first, normed, ws, pre_one, sem):
    load = pltpu.make_async_copy(ws_hbm, ws, sem)
    load.start()
    chan = low.shape[0] // (MEL_ROWS + 2)
    wide = low.shape[1]
    pre_one[...] = dot(w1[2 * chan : (MEL_ROWS + 4) * chan], x3[...])
    mean = jnp.broadcast_to(stats[0:chan, 0:1], (chan, wide))
    inv = jnp.broadcast_to(stats[0:chan, 1:2], (chan, wide))
    for q in range(MEL_ROWS + 2):
        at = slice(q * chan, (q + 1) * chan)
        mask = masks[0:1] * row_valid(q - 1, MEL_ROWS)
        normed[at, :] = ((pre_one[at, :] - mean) * inv * mask).astype(BF16)
    load.wait()
    first[...] = dot(ws[...], low[...])


def finish(recv, features, stats, k1t, first, normed, ws, params, masks,
           spec_hbm, kernel_one_hbm, kernel_two_hbm, gain_hbm, bias_hbm,
           table, spec_grad, kernel_one, kernel_two, gain_out, bias_out, sems):
    chan = params.shape[1]
    rows = MEL_ROWS
    wide = normed.shape[1]
    frame_dev = wide - RIM
    usable, behind, ahead = (masks[n : n + 1] for n in range(3))
    total = masks[3:4, 0:1]
    gain = params[0:1]
    count = recv.shape[0] // 14
    share = -(-9 * chan // count)
    lower = -(-share // 2)
    left = [recv[pl.ds(5 + p, count, stride=14), :] for p in range(lower)]
    whole = jnp.concatenate([v[:, :chan] for v in left] + [v[:, chan:] for v in left], axis=0)
    for t in range(9):
        kernel_two[t] = whole[t * chan : (t + 1) * chan].T
    stores = [pltpu.make_async_copy(kernel_two, kernel_two_hbm, sems.at[3])]
    stores[0].start()
    sums = summed_blocks(recv, count)[0:5]
    ten = jnp.concatenate([sums[:, :chan], sums[:, chan:]], axis=0)
    bias_sum = ten[9:10]
    mean_l, inv_l = stats[chan : chan + 1, :chan], stats[chan + 8 : chan + 9, :chan]
    ten = ten - features[1:2, 0:1] * bias_sum
    k = k1t[0:9]
    gain_sum = inv_l * (jnp.sum(k * ten[0:9], axis=0, keepdims=True) - mean_l * bias_sum)
    gain_out[...] = gain_sum
    bias_out[...] = bias_sum
    for n, (source, target) in enumerate(((gain_out, gain_hbm), (bias_out, bias_hbm))):
        stores.append(pltpu.make_async_copy(source, target, sems.at[n]))
        stores[-1].start()
    factor_l = gain * inv_l
    scale = factor_l * gain_sum / total
    scale = jnp.concatenate([scale, scale], axis=1)
    scale = jnp.concatenate([scale] * ((rows + 2) // 2), axis=1)
    taps = first[...] - dot((ws[...].astype(F32) * scale).astype(BF16), normed[...])
    for part in range(wide // 128):
        table[part] = taps[:, 128 * part : 128 * (part + 1)]
    moved = [
        jnp.concatenate([table[part, pl.ds(b, rows, stride=8), :] for part in range(wide // 128)], axis=1)
        for b in range(3)
    ]
    constant = jnp.sum(k * (factor_l * bias_sum / total), axis=1, keepdims=True)
    for a in range(3):
        row = iota((rows, 1), 0) + (a - 1) + lax.axis_index("mel") * rows
        valid = ((row >= 0) & (row < lax.axis_size("mel") * rows)).astype(F32) * usable
        for b in range(3):
            t = 3 * (2 - a) + 2 - b
            moved[b] = moved[b] - constant[t : t + 1] * valid
    result = pltpu.roll(moved[0], 1, 1) * behind + moved[1] + pltpu.roll(moved[2], wide - 1, 1) * ahead
    spec_grad[0] = (result * usable)[:, :frame_dev]
    stores.append(pltpu.make_async_copy(spec_grad, spec_hbm, sems.at[2]))
    stores[-1].start()
    row = features[0:1, :]
    lane = iota((1, 128), 1)
    gram = jnp.concatenate(
        [jnp.where(lane < 9, pltpu.roll(row, 128 - 9 * t, 1) if t else row, 0.0) for t in range(9)]
        + [jnp.zeros((7, 128), F32)],
        axis=0,
    )
    single = to_column(row, 16, 81)[0:9]
    k_rows = jnp.concatenate([k1t[...], jnp.zeros((112, chan), F32)], axis=0)
    normed_taps = inv_l * (dot(gram, k_rows, precision=EXACT)[0:9] - single * mean_l)
    grad_taps = factor_l * (ten[0:9] - (bias_sum * single + gain_sum * normed_taps) / total)
    for i in range(3):
        kernel_one[i] = grad_taps[3 * i : 3 * i + 3]
    stores.append(pltpu.make_async_copy(kernel_one, kernel_one_hbm, sems.at[4]))
    stores[-1].start()
    for store in stores:
        store.wait()


def run(kernel, outs, scratch, *args, hbm=0, apart=(), flops=10**8, size=4 * 10**6):
    vmem = pl.BlockSpec(memory_space=pltpu.VMEM)
    devices = lax.axis_size("mel") * lax.axis_size("tm")
    specs = []
    args = list(args)
    for n, a in enumerate(args):
        if hbm and n >= len(args) - hbm:
            specs.append(pl.BlockSpec(memory_space=pltpu.HBM))
            args[n] = pltpu.with_memory_space_constraint(a, pltpu.HBM)
        else:
            specs.append(vmem)
            args[n] = pltpu.with_memory_space_constraint(a, pltpu.VMEM)
    return pl.pallas_call(
        kernel,
        out_shape=outs,
        in_specs=specs,
        out_specs=[pl.BlockSpec(memory_space=pltpu.HBM) if n in apart else vmem for n in range(len(outs))],
        scratch_shapes=scratch,
        compiler_params=pltpu.CompilerParams(vmem_limit_bytes=(29 + devices // 32) * 2**20),
        cost_estimate=pl.CostEstimate(flops=flops, bytes_accessed=size, transcendentals=0),
    )(*args)


def shape(dims, dtype=F32):
    return jax.ShapeDtypeStruct(dims, dtype)


def kept(dims, dtype=F32):
    return pltpu.VMEM(dims, dtype)


def far(dims, dtype=F32):
    return pltpu.HBM(dims, dtype)


def exchange(blocks, axes=AXES):
    return lax.all_to_all(blocks, axes, 0, 0, tiled=True)


def exchange_rows(rows, axes=AXES):
    return exchange(rows[:, None, :], axes)[:, 0, :]


def shards(spectrum, clip_bounds, kernel_one, gain_one, bias_one, kernel_two, gain_two, bias_two, pooled_grad):
    _, rows, frame_dev = spectrum.shape
    chan = kernel_two.shape[0]
    n_mel, n_tm = lax.axis_size("mel"), lax.axis_size("tm")
    devices = n_mel * n_tm
    half = frame_dev // 2
    wide = frame_dev + RIM
    mels = n_mel * rows

    packed, own, spec, masks = run(
        pack,
        [
            kept((devices, FIRST, 128), BF16),
            kept(pooled_grad.shape, BF16),
            kept(spectrum.shape, BF16),
            kept((8, wide)),
        ],
        [
            pltpu.SMEM(clip_bounds.shape, jnp.int32),
            pltpu.VMEM((2 * chan, half), F32),
            pltpu.VMEM((devices * FIRST, 128), F32),
            pltpu.SemaphoreType.DMA((3,)),
        ],
        spectrum,
        pooled_grad,
        clip_bounds,
        hbm=3,
    )
    recv = exchange(packed)
    ext = rows + 6
    span = 4 * 3 * chan
    wf, wb, w1, ws, pairs, singles, k1t, params, all_masks, edge_masks, twice, own_rows = run(
        weights,
        [
            kept((2 * chan, span), BF16),
            kept((2 * chan, span), BF16),
            kept((ext * chan, 128), BF16),
            far((rows * 8, (rows + 2) * chan), BF16),
            kept((chan, 128)),
            kept((chan, 128)),
            kept((16, chan)),
            kept((8, chan)),
            kept((8, n_tm * frame_dev)),
            kept((n_tm * 8, 128)),
            kept((128, 128)),
            kept((chan * rows // 2, half), BF16),
        ],
        [
            pltpu.VMEM((9, chan, chan), BF16),
            pltpu.VMEM((3, 3, chan), BF16),
            pltpu.VMEM((4, 1, chan), F32),
            pltpu.SMEM(clip_bounds.shape, jnp.int32),
            pltpu.VMEM((rows * 8, (rows + 2) * chan), BF16),
            pltpu.VMEM((chan * rows // 2, half), F32),
            pltpu.SemaphoreType.DMA((8,)),
        ],
        own,
        clip_bounds,
        jnp.transpose(kernel_two, (2, 3, 0, 1)).reshape(9, chan, chan),
        jnp.transpose(kernel_one, (1, 2, 0)),
        gain_one[None],
        bias_one[None],
        gain_two[None],
        bias_two[None],
        hbm=7,
        apart=(3,),
    )
    pre_two, payload, act, x3, stats_one, features = run(
        forward_one,
        [
            kept(((rows + 4) * chan, wide)),
            kept((devices, SECOND, 128), BF16),
            kept((ext * 3 * chan, wide), BF16),
            kept((128, wide), BF16),
            kept((2 * chan + 16, 128)),
            kept((8, 128)),
        ],
        [
            pltpu.VMEM((ext * chan, wide), F32),
            pltpu.VMEM((devices * FIRST, 128), F32),
            pltpu.VMEM((n_tm * 8, 128), F32),
            pltpu.VMEM((mels + 8, RIM), F32),
            pltpu.VMEM((devices * SECOND, 128), F32),
        ],
        recv,
        spec,
        pairs,
        singles,
        twice,
        w1,
        wf,
        params,
        masks,
        all_masks,
        edge_masks,
    )
    recv = exchange(payload)
    grad, payload, stats_two = run(
        backward_scaled,
        [
            kept(((rows + 4) * chan, wide)),
            kept((devices * sum_rows(devices, 9 * chan), 128)),
            kept((chan + 8, 128)),
        ],
        [
            pltpu.VMEM(((rows // 2 + 2) * chan, RIM), F32),
            pltpu.VMEM((3 * chan + 16, rows * frame_dev), BF16),
            pltpu.VMEM((devices * SECOND, 128), F32),
            pltpu.VMEM((2 * chan, half), F32),
        ],
        recv,
        pre_two,
        act,
        own_rows,
        params,
        masks,
    )
    recv = exchange_rows(payload)
    low, payload, gain_two_grad, bias_two_grad, pre_two = run(
        backward,
        [
            kept(((rows + 2) * chan, wide), BF16),
            kept((devices * 14, 128)),
            shape((1, chan)),
            shape((1, chan)),
            far((rows * chan, wide)),
        ],
        [
            pltpu.VMEM(((rows + 4) * 3 * chan, wide), BF16),
            pltpu.VMEM(((rows + 2) * chan, wide), F32),
            pltpu.VMEM((rows * chan, frame_dev), F32),
            pltpu.SemaphoreType.DMA,
        ],
        recv,
        pre_two,
        grad,
        stats_two,
        w1,
        x3,
        stats_one,
        params,
        masks,
        wb,
        apart=(4,),
    )
    recv = exchange_rows(payload)
    (pooled,) = run(
        pool,
        [shape((1, chan, rows // 2, half), BF16)],
        [
            pltpu.VMEM((rows // 2 * chan, 128), F32),
            pltpu.VMEM((rows * chan, wide), F32),
            pltpu.SemaphoreType.DMA((2,)),
        ],
        payload,
        stats_two,
        masks,
        pre_two,
        hbm=1,
    )
    first, normed, ws = run(
        transposed,
        [
            kept((rows * 8, wide)),
            kept(((rows + 2) * chan, wide), BF16),
            kept((rows * 8, (rows + 2) * chan), BF16),
        ],
        [pltpu.VMEM(((rows + 2) * chan, wide), F32), pltpu.SemaphoreType.DMA],
        low,
        w1,
        x3,
        stats_one,
        masks,
        ws,
        hbm=1,
    )
    spec_grad, kernel_one_grad, kernel_two_grad, gain_one_grad, bias_one_grad = run(
        finish,
        [
            shape((1, rows, frame_dev)),
            shape((3, 3, chan)),
            shape((9, chan, chan)),
            shape((1, chan)),
            shape((1, chan)),
        ],
        [
            pltpu.VMEM((3, rows * 8, 128), F32),
            pltpu.VMEM((1, rows, frame_dev), F32),
            pltpu.VMEM((3, 3, chan), F32),
            pltpu.VMEM((9, chan, chan), F32),
            pltpu.VMEM((1, chan), F32),
            pltpu.VMEM((1, chan), F32),
            pltpu.SemaphoreType.DMA((5,)),
        ],
        recv,
        features,
        stats_one,
        k1t,
        first,
        normed,
        ws,
        params,
        masks,
        apart=range(5),
    )
    kernel_two_grad = jnp.transpose(kernel_two_grad.reshape(3, 3, chan, chan), (2, 3, 0, 1))
    return (
        pooled,
        spec_grad,
        jnp.transpose(kernel_one_grad, (2, 0, 1)),
        gain_one_grad[0],
        bias_one_grad[0],
        kernel_two_grad,
        gain_two_grad[0],
        bias_two_grad[0],
    )


def solution(mesh):
    return jax.shard_map(
        shards,
        mesh=mesh,
        in_specs=(
            P(None, "mel", "tm"),
            P(),
            P(),
            P(),
            P(),
            P(),
            P(),
            P(),
            P(None, None, "mel", "tm"),
        ),
        out_specs=(P(None, None, "mel", "tm"), P(None, "mel", "tm"), P(), P(), P(), P(), P(), P()),
        check_vma=False,
    )
```

```python
import math

import jax
import jax.numpy as jnp
from jax import lax
from jax.experimental import pallas as pl
from jax.experimental.pallas import tpu as pltpu
from jax.sharding import PartitionSpec as P

F32 = jnp.float32
BF16 = jnp.bfloat16
AXES = ("mel", "tm")
EXACT = lax.Precision.HIGHEST
RIM = 128
BAND = 24
MEL_ROWS = 16
FIRST = 24
SUMS, EDGES, COLUMNS = 16, 19, 23
SIDE = 96
SECOND = 8


def iota(shape, dim):
    return lax.broadcasted_iota(jnp.int32, shape, dim)


def dot(a, b, over=((1,), (0,)), precision=None):
    return lax.dot_general(a, b, (over, ((), ())), precision=precision, preferred_element_type=F32)


def to_column(lanes, count, start=0):
    shape = (count, lanes.shape[1])
    return jnp.sum(jnp.where(iota(shape, 1) == iota(shape, 0) + start, lanes, 0.0), axis=1, keepdims=True)


def to_lanes(column, start=0, width=128):
    shape = (column.shape[0], width)
    return jnp.sum(jnp.where(iota(shape, 1) == iota(shape, 0) + start, column, 0.0), axis=0, keepdims=True)


def halves(v):
    total = v[:, :128]
    for n in range(128, v.shape[1], 128):
        total = total + v[:, n : n + 128]
    return total


def frame_masks(bounds, frames):
    last = bounds.shape[1] - 1

    def living(f):
        return (f >= 0) & (f < bounds[0, last])

    def paired(f):
        both = living(f) & living(f + 1)
        for k in range(1, last):
            both = both & (f + 1 != bounds[0, k])
        return both

    return tuple(m.astype(F32) for m in (living(frames), paired(frames - 1), paired(frames)))


def row_valid(row, rows):
    mel = lax.axis_index("mel") * rows + row
    return ((mel >= 0) & (mel < lax.axis_size("mel") * rows)).astype(F32)


def start_all(*pairs, sems):
    copies = [pltpu.make_async_copy(src, dst, sems.at[n]) for n, (src, dst) in enumerate(pairs)]
    for copy in copies:
        copy.start()
    return copies


def wait_all(copies):
    for copy in copies:
        copy.wait()


def shifted_frames(value, behind, ahead):
    wide = value.shape[1]
    return pltpu.roll(value, 1, 1) * behind, pltpu.roll(value, wide - 1, 1) * ahead


def three_parts(v):
    high = lax.reduce_precision(v, 8, 7)
    mid = lax.reduce_precision(v - high, 8, 7)
    return high, mid, v - high - mid


def share_of(devices, chan):
    return -(-chan // devices)


def pack(spec_hbm, grad_hbm, bounds_hbm, out, own, spec, masks, bounds, edges, rows_out, sems):
    copies = start_all((bounds_hbm, bounds), (spec_hbm, spec), (grad_hbm, own), sems=sems)
    copies[0].wait()
    wide = masks.shape[1]
    frame_dev = wide - RIM
    devices = out.shape[0]
    rows = MEL_ROWS
    lane = iota((1, wide), 1)
    frames = lax.axis_index("tm") * frame_dev + jnp.where(lane < frame_dev + RIM // 2, lane, lane - wide)
    last = bounds.shape[1] - 1
    pixels = (bounds[0, last] * (lax.axis_size("mel") * rows)).astype(F32)
    found = frame_masks(bounds, frames)
    masks[...] = jnp.concatenate(
        list(found) + [jnp.full((1, wide), 1.0) * pixels, jnp.zeros((4, wide), F32)], axis=0
    )
    usable, behind, ahead = (m[:, :frame_dev] for m in found)
    copies[1].wait()
    x = spec[0].astype(F32) * usable
    lane = iota((1, frame_dev), 1)
    row = iota((rows, 1), 0)
    inner = jnp.where((lane > 0) & (lane < frame_dev - 1), usable, 0.0)
    number = (rows - 2) * jnp.sum(inner, axis=1, keepdims=True)
    inner = inner * ((row > 0) & (row < rows - 1)).astype(F32)
    centre = jnp.sum(jnp.sum(x, axis=0, keepdims=True), axis=1, keepdims=True)
    centre = centre / (rows * jnp.maximum(jnp.sum(usable, axis=1, keepdims=True), 1.0))
    centre = lax.reduce_precision(centre, 8, 7)
    shifted = [pltpu.roll(x, 1, 1) * behind, x, pltpu.roll(x, frame_dev - 1, 1) * ahead]
    taps = [pltpu.roll(v, (1 - i) % rows, 0) if i != 1 else v for i in range(3) for v in shifted]
    features = feature_rows(centre, (taps, inner))
    lane = iota((1, 128), 1)
    features = jnp.where(lane == 90, centre, jnp.where(lane == 91, number, features))
    pick = iota((8, frame_dev), 0)
    column = jnp.where(pick < 4, pick, frame_dev - 8 + pick)
    strip = dot((iota((8, frame_dev), 1) == column).astype(BF16), x.astype(BF16), ((1,), (1,)))
    lane = iota((8, 128), 1)
    repeat = (iota((rows, 128), 1) % rows == iota((rows, 128), 0)).astype(BF16)
    strip = jnp.where(lane // rows == iota((8, 128), 0), dot(strip.astype(BF16), repeat), 0.0)
    strip = jnp.sum(strip, axis=0, keepdims=True)

    def put(n, value):
        rows_out[pl.ds(n, devices, stride=FIRST), :] = jnp.broadcast_to(value, (devices, 128))

    near = jnp.concatenate([x[0:4], x[rows - 4 :]], axis=0)
    for n in range(8):
        put(n, near[n : n + 1, :128])
        put(8 + n, near[n : n + 1, 128:])
    put(COLUMNS, strip)
    copies[2].wait()
    _, chan, many, half = own.shape
    share = share_of(devices, chan)
    holders = chan // share
    g = own[0].astype(F32)
    edges[0:chan] = g[:, 0, :]
    edges[chan:] = g[:, many - 1, :]

    def spread_out(v):
        if holders < devices:
            v = jnp.concatenate([v, jnp.zeros((devices - holders, 128), F32)], axis=0)
        return v

    for n in range(share):
        put(EDGES + n, spread_out(edges[n * holders : (n + 1) * holders, :]))
        put(EDGES + share + n, spread_out(edges[chan + n * holders : chan + (n + 1) * holders, :]))
    for n in range(2 * share, COLUMNS - EDGES):
        put(EDGES + n, jnp.zeros((1, 128), F32))
    end = iota((8, half), 0)
    at = iota((8, half), 1)
    ends = ((end == 0) & (at == 0)) | ((end == 1) & (at == half - 1))
    columns = dot(ends.astype(BF16), g.reshape(chan * many, half).astype(BF16), ((1,), (1,)))
    group = 128 // many
    source = iota((128, 128), 0)
    lane = iota((group, 128), 1)
    mine = lane // many == iota((group, 128), 0)
    parts = three_parts(features)
    for n in range(2):
        side = jnp.zeros((holders, 128), F32)
        for m in range(share):
            move = (iota((128, 128), 1) == SIDE + many * m + source % many).astype(BF16)
            first = m * holders * many // 128
            block = [columns[n : n + 1, 128 * q : 128 * (q + 1)] for q in range(first, first + holders * many // 128)]
            block = jnp.concatenate([jnp.where(mine, v, 0.0) for v in block], axis=0)
            side = side + dot(block.astype(BF16), move)
        put(SUMS + n, spread_out(side) + parts[n])
    put(SUMS + 2, parts[2])
    out[...] = rows_out[...].reshape(out.shape).astype(BF16)


def weights(own, bounds_hbm, k2_hbm, k1_hbm, gain_one_hbm, bias_one_hbm, gain_two_hbm, bias_two_hbm,
            wf, wb, w1, ws_hbm, pairs, singles, k1t, params, all_masks, edge_masks, twice, own_rows,
            k2, k1, vectors, bounds, ws, temp, sems):
    loads = start_all(
        (bounds_hbm, bounds),
        (k2_hbm, k2),
        (k1_hbm, k1),
        (gain_one_hbm, vectors.at[0]),
        (bias_one_hbm, vectors.at[1]),
        (gain_two_hbm, vectors.at[2]),
        (bias_two_hbm, vectors.at[3]),
        sems=sems,
    )
    _, many, count, half = own.shape
    temp[...] = own[0].astype(F32).reshape(many * count, half)
    for r in range(count):
        own_rows[r * many : (r + 1) * many] = temp[pl.ds(r, many, stride=count), :].astype(BF16)
    wait_all(loads)
    chan = k2.shape[1]
    span = wf.shape[1]
    taps = [k2[t].astype(F32) for t in range(9)]
    rest = jnp.zeros((chan, span - 9 * chan), F32)
    forward = jnp.concatenate(taps + [rest], axis=1)
    backward = jnp.concatenate([taps[8 - t].T for t in range(9)] + [rest], axis=1)
    for r in range(wb.shape[0] // chan):
        at = slice(r * chan, (r + 1) * chan)
        wb[at] = (pltpu.roll(backward, 3 * chan * r, 1) if r else backward).astype(BF16)
    full = jnp.concatenate([k1[n].astype(F32) for n in range(3)] + [jnp.zeros((7, chan), F32)], axis=0)
    low = [
        jnp.concatenate([full[3 * (2 - a) + 2 - b : 3 * (2 - a) + 3 - b] for a in range(3)], axis=1)
        for b in range(3)
    ]
    base = jnp.concatenate(low + [jnp.zeros((5, 3 * chan), F32)], axis=0)
    base = jnp.concatenate([base, jnp.zeros((8, ws.shape[1] - 3 * chan), F32)], axis=1)
    for m in range(ws.shape[0] // 8):
        ws[8 * m : 8 * m + 8] = (pltpu.roll(base, chan * m, 1) if m else base).astype(BF16)
    store_ws = pltpu.make_async_copy(ws, ws_hbm, sems.at[7])
    store_ws.start()
    frames = all_masks.shape[1]
    frame_dev = frames // lax.axis_size("tm")
    all_masks[...] = jnp.concatenate(
        list(frame_masks(bounds, iota((1, frames), 1))) + [jnp.zeros((5, frames), F32)], axis=0
    )
    q = iota(edge_masks.shape, 0)
    lane = iota(edge_masks.shape, 1)
    k = q % 8
    frames = (q // 8) * frame_dev + jnp.where(k < 4, k, k + frame_dev - 8)
    living, behind, ahead = frame_masks(bounds, frames)
    living = jnp.where((k == 0) | (k == 7), living, 0.0)
    edge_masks[...] = jnp.where(lane == 0, living, jnp.where(lane == 1, behind, jnp.where(lane == 2, ahead, 0.0)))
    params[...] = jnp.concatenate(
        [vectors[n] for n in range(4)] + [jnp.zeros((4, chan), F32)], axis=0
    )
    tap = iota((16, 128), 0)
    lane = iota((16, 128), 1)
    i = (tap * 11) >> 5
    ninth = (lane * 57) >> 9
    to_band = (lane == BAND * (tap - 3 * i) + i) & (tap < 9)
    to_left = (ninth == tap) & (tap < 9)
    to_right = (lane - 9 * ninth == tap) & (lane < 81)
    to_single = (lane == 81 + tap) & (tap < 9)
    source = iota((128, 128), 0) - 81
    lane = iota((128, 128), 1)
    ninth = (lane * 57) >> 9
    inside = (source >= 0) & (source < 9) & (lane < 81)
    twice[...] = jnp.where(inside, (source == ninth).astype(F32) + (source == lane - 9 * ninth).astype(F32), 0.0)
    for r in range(wf.shape[0] // chan):
        at = slice(r * chan, (r + 1) * chan)
        wf[at] = (pltpu.roll(forward, 3 * chan * r, 1) if r else forward).astype(BF16)
    k1t[...] = full
    k = full.astype(BF16)
    lanes = [dot(k, select.astype(BF16), ((0,), (0,))) for select in (to_band, to_left, to_right, to_single)]
    pairs[...] = lanes[1] * lanes[2]
    singles[...] = lanes[3]
    for m in range(w1.shape[0] // chan):
        w1[m * chan : (m + 1) * chan] = (pltpu.roll(lanes[0], m, 1) if m else lanes[0]).astype(BF16)
    store_ws.wait()


def feature_rows(centre, *parts):
    def folded(v):
        return jnp.sum(halves(v), axis=0, keepdims=True)

    rows = [jnp.zeros((1, 128), F32)] * 96
    for taps, weight in parts:
        z = [tap - centre for tap in taps]
        for s in range(9):
            left = z[s] * weight
            rows[81 + s] = rows[81 + s] + folded(left)
            for t in range(s, 9):
                rows[9 * s + t] = rows[9 * t + s] = rows[9 * s + t] + folded(left * z[t])
    return to_lanes(jnp.sum(jnp.concatenate(rows, axis=0), axis=1, keepdims=True))


def summed_blocks(ref, devices):
    block = ref.shape[0] // devices
    period = 8 // math.gcd(block, 8)
    step = period * block
    total = ref[0:step, :]
    for at in range(step, ref.shape[0], step):
        total = total + ref[at : at + step, :]
    result = total[0:block]
    for n in range(1, period):
        result = result + total[n * block : (n + 1) * block]
    return result


def moved_rows(v, step):
    if step == 0:
        return v
    count = v.shape[0]
    if abs(step) >= count:
        return jnp.zeros_like(v)
    zero = jnp.zeros((abs(step), v.shape[1]), v.dtype)
    if step > 0:
        return jnp.concatenate([zero, v[: count - step]], axis=0)
    return jnp.concatenate([v[-step:], zero], axis=0)


def silu_halves(h):
    t = jnp.tanh(h)
    one = 1.0 + t
    return h * one, one * (1.0 + h * (1.0 - t))


def forward_one(recv, spec, pairs, singles, twice, w1, wf, params, masks, all_masks, edge_masks,
                pre_two, payload, act, x3, stats, features_out, pre_one, got, strips, halo, rows_out):
    devices = recv.shape[0]
    n_mel, count = lax.axis_size("mel"), lax.axis_size("tm")
    rows = MEL_ROWS
    mels = n_mel * rows
    wide = masks.shape[1]
    frame_dev = wide - RIM
    chan = params.shape[1]
    me_m, me_t = lax.axis_index("mel"), lax.axis_index("tm")
    usable, behind, ahead = (masks[n : n + 1] for n in range(3))
    total = masks[3:4, 0:1]
    got[...] = recv[...].astype(F32).reshape(devices * FIRST, 128)

    def every(n):
        return got[pl.ds(n, devices, stride=FIRST), :]

    lane = iota((count, 128), 1)
    bands = [got[pl.ds(FIRST * k * count + COLUMNS, count, stride=FIRST), :] for k in range(n_mel)]
    for c in range(8):
        column = jnp.zeros((count, 128), F32)
        for k, band in enumerate(bands):
            part = jnp.where(lane // rows == c, band, 0.0)
            column = column + (pltpu.roll(part, rows * (k - c) % 128, 1) if k != c else part)
        strips[pl.ds(c, count, stride=8), :] = column
    at = pl.multiple_of(FIRST * (jnp.maximum(me_m - 1, 0) * count + me_t), 8)
    above = got[pl.ds(at, 16), :] * (me_m > 0).astype(F32)
    at = pl.multiple_of(FIRST * (jnp.minimum(me_m + 1, n_mel - 1) * count + me_t), 8)
    below = got[pl.ds(at, 16), :] * (me_m < n_mel - 1).astype(F32)
    above = jnp.concatenate([above[4:8], above[12:16]], axis=1)
    below = jnp.concatenate([below[0:4], below[8:12]], axis=1)
    own = spec[0].astype(F32) * usable[:, :frame_dev]
    at = pl.multiple_of(8 * jnp.minimum(me_t + 1, count - 1), 8)
    after = strips[pl.ds(at, 8), :][:, :mels] * (me_t + 1 < count).astype(F32)
    at = pl.multiple_of(8 * jnp.maximum(me_t - 1, 0), 8)
    before = strips[pl.ds(at, 8), :][:, :mels] * (me_t > 0).astype(F32)
    sides = jnp.concatenate([after[0:4], before[4:8], jnp.zeros((8, mels), F32)], axis=0).astype(BF16)
    side = iota((16, RIM), 0)
    place = iota((16, RIM), 1) == jnp.where(side < 4, side, jnp.where(side < 8, side + RIM - 8, -1))
    halo[0:8] = jnp.zeros((8, RIM), F32)
    halo[mels : mels + 8] = jnp.zeros((8, RIM), F32)
    halo[4 : mels + 4] = dot(sides, place.astype(BF16), ((0,), (0,)))
    rim = halo[pl.ds(pl.multiple_of(me_m * rows, 8), BAND), :]
    near = jnp.concatenate([jnp.concatenate([above, own, below], axis=0), rim], axis=1)
    x3[...] = jnp.concatenate(
        [
            pltpu.roll(near, 1, 1) * behind,
            near,
            pltpu.roll(near, wide - 1, 1) * ahead,
            jnp.broadcast_to(usable, (BAND, wide)),
            jnp.zeros((128 - 4 * BAND, wide), F32),
        ],
        axis=0,
    ).astype(BF16)
    pre_one[...] = dot(w1[...], x3[...])
    lane = iota((1, 128), 1)
    parts = jnp.where(lane < 92, every(SUMS) + every(SUMS + 1) + every(SUMS + 2), 0.0)
    centres, numbers = parts[:, 90:91], parts[:, 91:92]
    centre = jnp.sum(centres * numbers, axis=0, keepdims=True)
    centre = centre / jnp.maximum(jnp.sum(numbers, axis=0, keepdims=True), 1.0)
    delta = centres - centre
    features = jnp.sum(parts + delta * numbers * jnp.where(lane < 81, delta, 1.0), axis=0, keepdims=True)
    moved = jnp.sum(delta * parts, axis=0, keepdims=True)
    moved = dot(jnp.broadcast_to(moved, (8, 128)), twice[...], precision=EXACT)[0:1]
    features = features + moved
    tiles = []
    for k in range(n_mel):
        lanes = []
        for d in range(count):
            at = FIRST * (k * count + d)
            lanes += [got[at : at + 8, :], got[at + 8 : at + 16, :]]
        tiles.append(jnp.concatenate(lanes, axis=1))
    zero = jnp.zeros((1, tiles[0].shape[1]), F32)
    before_row, this_row, next_row = [], [], []
    for k, tile in enumerate(tiles):
        before_row += [tiles[k - 1][7:8] if k else zero, tile[6:7]]
        this_row += [tile[0:1], tile[7:8]]
        next_row += [tile[1:2], tiles[k + 1][0:1] if k + 1 < n_mel else zero]
    f_usable, f_behind, f_ahead = (all_masks[n : n + 1] for n in range(3))
    taps = []
    for group in (before_row, this_row, next_row):
        v = jnp.concatenate(group, axis=0)
        taps += [pltpu.roll(v, 1, 1) * f_behind, v, pltpu.roll(v, v.shape[1] - 1, 1) * f_ahead]
    borders = (taps, f_usable)
    edge = strips[...]
    q_usable, q_behind, q_ahead = (edge_masks[:, n : n + 1] for n in range(3))
    lane = iota((count * 8, 128), 1)
    inside = (lane < mels) & (lane % rows != 0) & (lane % rows != rows - 1)
    shifted = [
        pltpu.roll(edge, 1, 0) * q_behind,
        edge,
        pltpu.roll(edge, count * 8 - 1, 0) * q_ahead,
    ]
    taps = [pltpu.roll(v, (1 - i) % 128, 1) if i != 1 else v for i in range(3) for v in shifted]
    features = features + feature_rows(centre, borders, (taps, jnp.where(inside, q_usable, 0.0)))
    features = jnp.where(iota((1, 128), 1) < 90, features, 0.0)
    features_out[...] = jnp.concatenate(
        [features, jnp.broadcast_to(centre, (1, 128)), jnp.zeros((6, 128), F32)], axis=0
    )
    near_mean = jnp.sum(singles[...] * features, axis=1, keepdims=True) / total
    square = jnp.sum(pairs[...] * features, axis=1, keepdims=True) / total
    inv = lax.rsqrt(square - near_mean * near_mean + 1e-05)
    mean = near_mean + centre * jnp.sum(singles[...], axis=1, keepdims=True)
    lane = iota((chan, 128), 1)
    stats[0:chan] = jnp.where(lane == 0, mean, jnp.where(lane == 1, inv, 0.0))
    stats[chan : chan + 8] = jnp.broadcast_to(to_lanes(near_mean), (8, 128))
    stats[chan + 8 : chan + 16] = jnp.broadcast_to(to_lanes(inv), (8, 128))
    scale = 0.5 * to_column(params[0:1], chan) * inv
    shift = 0.5 * to_column(params[1:2], chan) - mean * scale
    stats[chan + 16 :] = jnp.where(lane == 0, scale, jnp.where(lane == 1, shift, 0.0))
    scale = jnp.broadcast_to(scale, (chan, wide))
    shift = jnp.broadcast_to(shift, (chan, wide))
    ext = w1.shape[0] // chan
    block, taps = wf.shape
    first = jnp.zeros((chan, 128), F32)
    second = jnp.zeros((chan, 128), F32)
    own_mask = usable[:, :frame_dev]
    low_masks = [m.astype(BF16) for m in (usable, behind, ahead)]
    for r in range(ext):
        value, _ = silu_halves(pre_one[r * chan : (r + 1) * chan, :] * scale + shift)
        if not 0 <= r - 3 < rows:
            value = value * row_valid(r - 3, rows)
        base = r * 3 * chan
        low = value.astype(BF16) * low_masks[0]
        act[base : base + chan, :], act[base + 2 * chan : base + 3 * chan, :] = shifted_frames(low, *low_masks[1:])
        act[base + chan : base + 2 * chan, :] = low
        if r < 3 or r % 2 == 0:
            continue
        g = (r - 3) // 2
        result = dot(wf[...], act[g * 3 * block : g * 3 * block + taps, :])
        pre_two[g * block : (g + 1) * block] = result
        for q in range(2):
            if 2 <= 2 * g + q < rows + 2:
                p = result[q * chan : (q + 1) * chan, :frame_dev]
                masked = p * own_mask
                first = first + halves(masked)
                second = second + halves(masked * p)
    share = share_of(devices, chan)

    def put(n, value):
        rows_out[pl.ds(n, devices, stride=SECOND), :] = jnp.broadcast_to(value, (devices, 128))

    for n in range(share):
        put(3 + n, moved_rows(every(EDGES + share + n), count))
        put(3 + share + n, moved_rows(every(EDGES + n), -count))
    for n in range(3 + 2 * share, SECOND - 1):
        put(n, jnp.zeros((1, 128), F32))
    lane = iota((devices, 128), 1)
    tm = iota((devices, 128), 0) % count
    lefts = jnp.where(lane >= SIDE, every(SUMS), 0.0)
    rights = jnp.where(lane >= SIDE, every(SUMS + 1), 0.0)
    beside = jnp.zeros((devices, 128), F32)
    for n, step in enumerate((0, count, -count)):
        one = jnp.where(tm > 0, moved_rows(rights, step + 1), 0.0)
        two = jnp.where(tm < count - 1, moved_rows(lefts, step - 1), 0.0)
        beside = beside + pltpu.roll(one, (32 * n - SIDE) % 128, 1) + pltpu.roll(two, (32 * n + 16 - SIDE) % 128, 1)
    put(SECOND - 1, beside)
    first = jnp.sum(first, axis=1, keepdims=True)
    second = jnp.sum(second, axis=1, keepdims=True)
    for n, part in enumerate(three_parts(to_lanes(first) + to_lanes(second, chan))):
        put(n, part)
    payload[...] = rows_out[...].reshape(payload.shape).astype(BF16)


def sum_rows(devices, taps):
    return -(-taps // devices) + 2


def backward_scaled(recv, pre_two, act, own_rows, params, masks,
                    grad, payload, pairs, stats, sides, right, got, beyond):
    devices = recv.shape[0]
    got[...] = recv[...].astype(F32).reshape(devices * SECOND, 128)
    chan = params.shape[1]
    half = own_rows.shape[1]
    lane = iota((half, 2 * half), 1)
    spread = jnp.where(lane >> 1 == iota((half, 2 * half), 0), 0.25, 0.0).astype(BF16)
    rows = MEL_ROWS
    wide = pre_two.shape[1]
    frame_dev = wide - RIM
    usable = masks[0:1]
    share = share_of(devices, chan)
    holders = chan // share

    def every(n):
        return got[pl.ds(n, devices, stride=SECOND), :]

    beside = every(SECOND - 1)[:holders]
    lane = iota((holders, RIM), 1)
    many = rows // 2
    for n in range(share):
        first = n * holders
        beyond[first : first + holders, :] = every(3 + n)[:holders]
        beyond[chan + first : chan + first + holders, :] = every(3 + share + n)[:holders]
        for r in range(many + 2):
            at = many * n + (r if r < many else 32 + many - 1 if r == many else 64)
            left, right_of = beside[:, at : at + 1], beside[:, at + 16 : at + 17]
            side = jnp.where(lane >= RIM - 2, 0.25 * left, jnp.where(lane < 2, 0.25 * right_of, 0.0))
            sides[r * chan + first : r * chan + first + holders, :] = side
    total = masks[3:4, 0:1]
    sums = jnp.sum(every(0) + every(1) + every(2), axis=0, keepdims=True)
    mean = to_column(sums, chan) / total
    inv = lax.rsqrt(to_column(sums, chan, chan) / total - mean * mean + 1e-05)
    lane = iota((chan, 128), 1)
    scale = 0.5 * to_column(params[2:3], chan) * inv
    shift = 0.5 * to_column(params[3:4], chan) - mean * scale
    columns = jnp.zeros((chan, 128), F32)
    for n, column in enumerate((mean, inv, scale, shift)):
        columns = jnp.where(lane == n, column, columns)
    stats[0:chan] = columns
    stats[chan : chan + 8] = jnp.broadcast_to(to_lanes(inv), (8, 128))
    shift = jnp.broadcast_to(shift, (chan, wide))
    scale = jnp.broadcast_to(scale, (chan, wide))
    mean = jnp.broadcast_to(mean, (chan, frame_dev))
    inv = jnp.broadcast_to(inv, (chan, frame_dev))
    first = jnp.zeros((chan, 128), F32)
    second = jnp.zeros((chan, 128), F32)
    own_mask = usable[:, :frame_dev]
    right[3 * chan :] = jnp.ones((16, rows * frame_dev), BF16)
    table = jnp.zeros((9 * chan, 3 * chan + 16), F32)
    for q in list(range(2, rows + 2)) + [0, 1, rows + 2, rows + 3]:
        r = q // 2
        at = slice(q * chan, (q + 1) * chan)
        m = q - 2
        mask = 0.5 * usable if 0 <= m < rows else usable * (0.5 * row_valid(m, rows))
        if q % 2 == 0:
            if 1 <= r <= rows // 2:
                pooled, at_side = own_rows[(r - 1) * chan : r * chan], (r - 1) * chan
            elif r == 0:
                pooled, at_side = beyond[0:chan].astype(BF16), many * chan
            else:
                pooled, at_side = beyond[chan:].astype(BF16), (many + 1) * chan
            up = jnp.concatenate([dot(pooled, spread), sides[at_side : at_side + chan, :]], axis=1)
        pre = pre_two[at, :]
        value, slope = silu_halves(pre * scale + shift)
        g = up * slope * mask
        grad[at, :] = g
        if not 0 <= m < rows:
            continue
        g = g[:, :frame_dev]
        normed = (pre[:, :frame_dev] - mean) * inv
        first = first + halves(g * normed)
        second = second + halves(g)
        value = value[:, :frame_dev] * own_mask
        both = value if m % 2 == 0 else both + value
        if m % 2:
            pairs[(r - 1) * chan : r * chan, :] = both
        lanes = slice(m * frame_dev, (m + 1) * frame_dev)
        high = lax.reduce_precision(g, 8, 7)
        right[0:chan, lanes] = high.astype(BF16)
        right[chan : 2 * chan, lanes] = (g - high).astype(BF16)
        right[2 * chan : 3 * chan, lanes] = normed.astype(BF16)
        if m % 4 == 3:
            left = [act[(n + 2) * 3 * chan : (n + 5) * 3 * chan, :frame_dev] for n in range(m - 3, m + 1)]
            lanes = slice((m - 3) * frame_dev, (m + 1) * frame_dev)
            table = table + dot(jnp.concatenate(left, axis=1), right[:, lanes], ((1,), (1,)))
    first = jnp.sum(first, axis=1, keepdims=True)
    second = jnp.sum(second, axis=1, keepdims=True)
    totals = to_lanes(first) + to_lanes(second, chan)
    block = payload.shape[0] // devices
    payload[pl.ds(0, devices, stride=block), :] = jnp.broadcast_to(totals, (devices, 128))
    both = jnp.concatenate([table[:, :chan] + table[:, chan : 2 * chan], table[:, 2 * chan : 3 * chan]], axis=1)
    single = table[:, 3 * chan : 3 * chan + 1]
    lane = iota((devices, 128), 1)
    constants = jnp.zeros((devices, 128), F32)
    for k in range(block - 2):
        cut, ones = both[k * devices : (k + 1) * devices], single[k * devices : (k + 1) * devices]
        short = devices - cut.shape[0]
        if short:
            cut = jnp.concatenate([cut, jnp.zeros((short, 128), F32)], axis=0)
            ones = jnp.concatenate([ones, jnp.zeros((short, 1), F32)], axis=0)
        payload[pl.ds(1 + k, devices, stride=block), :] = cut
        constants = jnp.where(lane == k, ones, constants)
    payload[pl.ds(block - 1, devices, stride=block), :] = constants


def pool(after, pairs, out, temp):
    del after
    chan, rows, half = out.shape[1:]
    to_mean = jnp.where(iota((2 * half, half), 0) >> 1 == iota((2 * half, half), 1), 0.25, 0.0)
    pooled = dot(pairs[...], to_mean, precision=EXACT)
    for r in range(rows):
        temp[pl.ds(r, chan, stride=rows), :] = pooled[r * chan : (r + 1) * chan]
    out[0] = temp[...].reshape(chan, rows, half).astype(BF16)


def backward(recv, pre_two, grad, stats_two, w1, x3, stats, params, masks, wb,
             out, payload, gain_out, bias_out, g3, pre_one, g1):
    chan = params.shape[1]
    rows = MEL_ROWS
    wide = pre_two.shape[1]
    frame_dev = wide - RIM
    usable = masks[0:1]
    behind, ahead = (masks[n : n + 1].astype(BF16) for n in (1, 2))
    total = masks[3:4, 0:1]
    devices = payload.shape[0] // 14
    pre_one[...] = dot(w1[2 * chan : (rows + 4) * chan], x3[...])

    received = summed_blocks(recv, devices)
    sums = received[0:1]
    gain_sum, bias_sum = sums[:, :chan], sums[:, chan:]
    gain_out[...] = gain_sum
    bias_out[...] = bias_sum
    mean, inv = stats_two[0:chan, 0:1], stats_two[0:chan, 1:2]
    factor = to_column(params[2:3], chan) * inv
    gain_part = factor * (to_column(sums, chan) / total * inv)
    bias_part = factor * (to_column(sums, chan, chan) / total) - mean * gain_part
    gain_part = jnp.broadcast_to(gain_part, (chan, wide))
    bias_part = jnp.broadcast_to(bias_part, (chan, wide))
    factor = jnp.broadcast_to(factor, (chan, wide))
    scale = jnp.broadcast_to(stats[chan + 16 :, 0:1], (chan, wide))
    shift = jnp.broadcast_to(stats[chan + 16 :, 1:2], (chan, wide))
    factor_one = jnp.broadcast_to(to_column(params[0:1], chan) * stats[0:chan, 1:2], (chan, wide))
    count = pre_two.shape[0] // chan
    table = jnp.zeros((chan, 128), F32)
    for q in range(count):
        at = slice(q * chan, (q + 1) * chan)
        mask = usable if 0 <= q - 2 < rows else usable * row_valid(q - 2, rows)
        low = (factor * grad[at, :] - (bias_part + pre_two[at, :] * gain_part) * mask).astype(BF16)
        base = q * 3 * chan
        g3[base : base + chan, :], g3[base + 2 * chan : base + 3 * chan, :] = shifted_frames(low, behind, ahead)
        g3[base + chan : base + 2 * chan, :] = low
        if q < 3 or q % 2 == 0:
            continue
        start = q - 3
        result = dot(wb[...], g3[start * 3 * chan : (start + 4) * 3 * chan, :])
        for n in range(2):
            m = start + n - 1
            at = slice((m + 1) * chan, (m + 2) * chan)
            _, slope = silu_halves(pre_one[at, :] * scale + shift)
            mask = 0.5 * usable if 0 <= m < rows else usable * (0.5 * row_valid(m, rows))
            value = result[n * chan : (n + 1) * chan] * slope * mask
            out[at, :] = (value * factor_one).astype(BF16)
            if not 0 <= m < rows:
                continue
            g1[m * chan : (m + 1) * chan, :] = value[:, :frame_dev]
            if m % 4 == 3:
                part = g1[(m - 3) * chan : (m + 1) * chan, :]
                high = lax.reduce_precision(part, 8, 7)
                low = (part - high).astype(BF16)
                taps_in = x3[:, :frame_dev]
                products = dot(high.astype(BF16), taps_in, ((1,), (1,))) + dot(low, taps_in, ((1,), (1,)))
                for k in range(4):
                    table = table + pltpu.roll(products[k * chan : (k + 1) * chan], 128 - (m + k), 1)
    tap = iota((16, 128), 0)
    lane = iota((16, 128), 1)
    i = (tap * 11) >> 5
    select = ((lane == BAND * (tap - 3 * i) + i) & (tap < 9)) | ((lane == 3 * BAND) & (tap == 9))
    rows10 = dot(select.astype(F32), table, ((1,), (1,)), EXACT)
    share = received.shape[0] - 2
    mine = received[1 : share + 1]
    single = to_column(received[share + 1 :], share)
    factor_l = params[2:3] * stats_two[chan : chan + 1, :chan]
    mine = mine[:, :chan] - (bias_sum * single + gain_sum * mine[:, chan:]) / total
    mine = factor_l * mine
    lower = -(-share // 2)
    mine = jnp.concatenate([mine] + [jnp.zeros((2 * lower - share, chan), F32)] * (share % 2), axis=0)
    mine = jnp.concatenate([mine[:lower], mine[lower:]], axis=1)
    if lower < 9:
        mine = jnp.concatenate([mine, jnp.zeros((9 - lower, 128), F32)], axis=0)
    sums = jnp.concatenate([rows10[0:5], rows10[5:10]], axis=1)
    block = jnp.concatenate([sums, mine], axis=0)
    for d in range(devices):
        payload[14 * d : 14 * (d + 1), :] = block


def transposed(low, w1, x3, stats, masks, ws_hbm, first, normed, ws, pre_one, sem):
    load = pltpu.make_async_copy(ws_hbm, ws, sem)
    load.start()
    chan = low.shape[0] // (MEL_ROWS + 2)
    wide = low.shape[1]
    pre_one[...] = dot(w1[2 * chan : (MEL_ROWS + 4) * chan], x3[...])
    mean = jnp.broadcast_to(stats[0:chan, 0:1], (chan, wide))
    inv = jnp.broadcast_to(stats[0:chan, 1:2], (chan, wide))
    for q in range(MEL_ROWS + 2):
        at = slice(q * chan, (q + 1) * chan)
        mask = masks[0:1] * row_valid(q - 1, MEL_ROWS)
        normed[at, :] = ((pre_one[at, :] - mean) * inv * mask).astype(BF16)
    load.wait()
    first[...] = dot(ws[...], low[...])


def finish(recv, features, stats, k1t, first, normed, ws, params, masks,
           spec_hbm, kernel_one_hbm, kernel_two_hbm, gain_hbm, bias_hbm,
           table, spec_grad, kernel_one, kernel_two, gain_out, bias_out, sems):
    chan = params.shape[1]
    rows = MEL_ROWS
    wide = normed.shape[1]
    frame_dev = wide - RIM
    usable, behind, ahead = (masks[n : n + 1] for n in range(3))
    total = masks[3:4, 0:1]
    gain = params[0:1]
    count = recv.shape[0] // 14
    share = -(-9 * chan // count)
    lower = -(-share // 2)
    left = [recv[pl.ds(5 + p, count, stride=14), :] for p in range(lower)]
    whole = jnp.concatenate([v[:, :chan] for v in left] + [v[:, chan:] for v in left], axis=0)
    for t in range(9):
        kernel_two[t] = whole[t * chan : (t + 1) * chan].T
    stores = [pltpu.make_async_copy(kernel_two, kernel_two_hbm, sems.at[3])]
    stores[0].start()
    sums = summed_blocks(recv, count)[0:5]
    ten = jnp.concatenate([sums[:, :chan], sums[:, chan:]], axis=0)
    bias_sum = ten[9:10]
    mean_l, inv_l = stats[chan : chan + 1, :chan], stats[chan + 8 : chan + 9, :chan]
    ten = ten - features[1:2, 0:1] * bias_sum
    k = k1t[0:9]
    gain_sum = inv_l * (jnp.sum(k * ten[0:9], axis=0, keepdims=True) - mean_l * bias_sum)
    gain_out[...] = gain_sum
    bias_out[...] = bias_sum
    for n, (source, target) in enumerate(((gain_out, gain_hbm), (bias_out, bias_hbm))):
        stores.append(pltpu.make_async_copy(source, target, sems.at[n]))
        stores[-1].start()
    factor_l = gain * inv_l
    scale = factor_l * gain_sum / total
    scale = jnp.concatenate([scale, scale], axis=1)
    scale = jnp.concatenate([scale] * ((rows + 2) // 2), axis=1)
    taps = first[...] - dot((ws[...].astype(F32) * scale).astype(BF16), normed[...])
    for part in range(wide // 128):
        table[part] = taps[:, 128 * part : 128 * (part + 1)]
    moved = [
        jnp.concatenate([table[part, pl.ds(b, rows, stride=8), :] for part in range(wide // 128)], axis=1)
        for b in range(3)
    ]
    constant = jnp.sum(k * (factor_l * bias_sum / total), axis=1, keepdims=True)
    for a in range(3):
        row = iota((rows, 1), 0) + (a - 1) + lax.axis_index("mel") * rows
        valid = ((row >= 0) & (row < lax.axis_size("mel") * rows)).astype(F32) * usable
        for b in range(3):
            t = 3 * (2 - a) + 2 - b
            moved[b] = moved[b] - constant[t : t + 1] * valid
    result = pltpu.roll(moved[0], 1, 1) * behind + moved[1] + pltpu.roll(moved[2], wide - 1, 1) * ahead
    spec_grad[0] = (result * usable)[:, :frame_dev]
    stores.append(pltpu.make_async_copy(spec_grad, spec_hbm, sems.at[2]))
    stores[-1].start()
    row = features[0:1, :]
    lane = iota((1, 128), 1)
    gram = jnp.concatenate(
        [jnp.where(lane < 9, pltpu.roll(row, 128 - 9 * t, 1) if t else row, 0.0) for t in range(9)]
        + [jnp.zeros((7, 128), F32)],
        axis=0,
    )
    single = to_column(row, 16, 81)[0:9]
    k_rows = jnp.concatenate([k1t[...], jnp.zeros((112, chan), F32)], axis=0)
    normed_taps = inv_l * (dot(gram, k_rows, precision=EXACT)[0:9] - single * mean_l)
    grad_taps = factor_l * (ten[0:9] - (bias_sum * single + gain_sum * normed_taps) / total)
    for i in range(3):
        kernel_one[i] = grad_taps[3 * i : 3 * i + 3]
    stores.append(pltpu.make_async_copy(kernel_one, kernel_one_hbm, sems.at[4]))
    stores[-1].start()
    for store in stores:
        store.wait()


def run(kernel, outs, scratch, *args, hbm=0, apart=(), flops=10**8, size=4 * 10**6):
    vmem = pl.BlockSpec(memory_space=pltpu.VMEM)
    devices = lax.axis_size("mel") * lax.axis_size("tm")
    specs = []
    args = list(args)
    for n, a in enumerate(args):
        if hbm and n >= len(args) - hbm:
            specs.append(pl.BlockSpec(memory_space=pltpu.HBM))
            args[n] = pltpu.with_memory_space_constraint(a, pltpu.HBM)
        else:
            specs.append(vmem)
            args[n] = pltpu.with_memory_space_constraint(a, pltpu.VMEM)
    return pl.pallas_call(
        kernel,
        out_shape=outs,
        in_specs=specs,
        out_specs=[pl.BlockSpec(memory_space=pltpu.HBM) if n in apart else vmem for n in range(len(outs))],
        scratch_shapes=scratch,
        compiler_params=pltpu.CompilerParams(vmem_limit_bytes=(29 + devices // 32) * 2**20),
        cost_estimate=pl.CostEstimate(flops=flops, bytes_accessed=size, transcendentals=0),
    )(*args)


def shape(dims, dtype=F32):
    return jax.ShapeDtypeStruct(dims, dtype)


def kept(dims, dtype=F32):
    return pltpu.VMEM(dims, dtype)


def far(dims, dtype=F32):
    return pltpu.HBM(dims, dtype)


def exchange(blocks, axes=AXES):
    return lax.all_to_all(blocks, axes, 0, 0, tiled=True)


def exchange_rows(rows, axes=AXES):
    return exchange(rows[:, None, :], axes)[:, 0, :]


def shards(spectrum, clip_bounds, kernel_one, gain_one, bias_one, kernel_two, gain_two, bias_two, pooled_grad):
    _, rows, frame_dev = spectrum.shape
    chan = kernel_two.shape[0]
    n_mel, n_tm = lax.axis_size("mel"), lax.axis_size("tm")
    devices = n_mel * n_tm
    half = frame_dev // 2
    wide = frame_dev + RIM
    mels = n_mel * rows

    packed, own, spec, masks = run(
        pack,
        [
            kept((devices, FIRST, 128), BF16),
            kept(pooled_grad.shape, BF16),
            kept(spectrum.shape, BF16),
            kept((8, wide)),
        ],
        [
            pltpu.SMEM(clip_bounds.shape, jnp.int32),
            pltpu.VMEM((2 * chan, half), F32),
            pltpu.VMEM((devices * FIRST, 128), F32),
            pltpu.SemaphoreType.DMA((3,)),
        ],
        spectrum,
        pooled_grad,
        clip_bounds,
        hbm=3,
    )
    recv = exchange(packed)
    ext = rows + 6
    span = 4 * 3 * chan
    wf, wb, w1, ws, pairs, singles, k1t, params, all_masks, edge_masks, twice, own_rows = run(
        weights,
        [
            kept((2 * chan, span), BF16),
            kept((2 * chan, span), BF16),
            kept((ext * chan, 128), BF16),
            far((rows * 8, (rows + 2) * chan), BF16),
            kept((chan, 128)),
            kept((chan, 128)),
            kept((16, chan)),
            kept((8, chan)),
            kept((8, n_tm * frame_dev)),
            kept((n_tm * 8, 128)),
            kept((128, 128)),
            kept((chan * rows // 2, half), BF16),
        ],
        [
            pltpu.VMEM((9, chan, chan), BF16),
            pltpu.VMEM((3, 3, chan), BF16),
            pltpu.VMEM((4, 1, chan), F32),
            pltpu.SMEM(clip_bounds.shape, jnp.int32),
            pltpu.VMEM((rows * 8, (rows + 2) * chan), BF16),
            pltpu.VMEM((chan * rows // 2, half), F32),
            pltpu.SemaphoreType.DMA((8,)),
        ],
        own,
        clip_bounds,
        jnp.transpose(kernel_two, (2, 3, 0, 1)).reshape(9, chan, chan),
        jnp.transpose(kernel_one, (1, 2, 0)),
        gain_one[None],
        bias_one[None],
        gain_two[None],
        bias_two[None],
        hbm=7,
        apart=(3,),
    )
    pre_two, payload, act, x3, stats_one, features = run(
        forward_one,
        [
            kept(((rows + 4) * chan, wide)),
            kept((devices, SECOND, 128), BF16),
            kept((ext * 3 * chan, wide), BF16),
            kept((128, wide), BF16),
            kept((2 * chan + 16, 128)),
            kept((8, 128)),
        ],
        [
            pltpu.VMEM((ext * chan, wide), F32),
            pltpu.VMEM((devices * FIRST, 128), F32),
            pltpu.VMEM((n_tm * 8, 128), F32),
            pltpu.VMEM((mels + 8, RIM), F32),
            pltpu.VMEM((devices * SECOND, 128), F32),
        ],
        recv,
        spec,
        pairs,
        singles,
        twice,
        w1,
        wf,
        params,
        masks,
        all_masks,
        edge_masks,
    )
    recv = exchange(payload)
    grad, payload, row_pairs, stats_two = run(
        backward_scaled,
        [
            kept(((rows + 4) * chan, wide)),
            kept((devices * sum_rows(devices, 9 * chan), 128)),
            kept((rows // 2 * chan, frame_dev)),
            kept((chan + 8, 128)),
        ],
        [
            pltpu.VMEM(((rows // 2 + 2) * chan, RIM), F32),
            pltpu.VMEM((3 * chan + 16, rows * frame_dev), BF16),
            pltpu.VMEM((devices * SECOND, 128), F32),
            pltpu.VMEM((2 * chan, half), F32),
        ],
        recv,
        pre_two,
        act,
        own_rows,
        params,
        masks,
    )
    recv = exchange_rows(payload)
    low, payload, gain_two_grad, bias_two_grad = run(
        backward,
        [
            kept(((rows + 2) * chan, wide), BF16),
            kept((devices * 14, 128)),
            shape((1, chan)),
            shape((1, chan)),
        ],
        [
            pltpu.VMEM(((rows + 4) * 3 * chan, wide), BF16),
            pltpu.VMEM(((rows + 2) * chan, wide), F32),
            pltpu.VMEM((rows * chan, frame_dev), F32),
        ],
        recv,
        pre_two,
        grad,
        stats_two,
        w1,
        x3,
        stats_one,
        params,
        masks,
        wb,
    )
    recv = exchange_rows(payload)
    (pooled,) = run(
        pool,
        [shape((1, chan, rows // 2, half), BF16)],
        [
            pltpu.VMEM((rows // 2 * chan, 128), F32),
        ],
        payload,
        row_pairs,
    )
    first, normed, ws = run(
        transposed,
        [
            kept((rows * 8, wide)),
            kept(((rows + 2) * chan, wide), BF16),
            kept((rows * 8, (rows + 2) * chan), BF16),
        ],
        [pltpu.VMEM(((rows + 2) * chan, wide), F32), pltpu.SemaphoreType.DMA],
        low,
        w1,
        x3,
        stats_one,
        masks,
        ws,
        hbm=1,
    )
    spec_grad, kernel_one_grad, kernel_two_grad, gain_one_grad, bias_one_grad = run(
        finish,
        [
            shape((1, rows, frame_dev)),
            shape((3, 3, chan)),
            shape((9, chan, chan)),
            shape((1, chan)),
            shape((1, chan)),
        ],
        [
            pltpu.VMEM((3, rows * 8, 128), F32),
            pltpu.VMEM((1, rows, frame_dev), F32),
            pltpu.VMEM((3, 3, chan), F32),
            pltpu.VMEM((9, chan, chan), F32),
            pltpu.VMEM((1, chan), F32),
            pltpu.VMEM((1, chan), F32),
            pltpu.SemaphoreType.DMA((5,)),
        ],
        recv,
        features,
        stats_one,
        k1t,
        first,
        normed,
        ws,
        params,
        masks,
        apart=range(5),
    )
    kernel_two_grad = jnp.transpose(kernel_two_grad.reshape(3, 3, chan, chan), (2, 3, 0, 1))
    return (
        pooled,
        spec_grad,
        jnp.transpose(kernel_one_grad, (2, 0, 1)),
        gain_one_grad[0],
        bias_one_grad[0],
        kernel_two_grad,
        gain_two_grad[0],
        bias_two_grad[0],
    )


def solution(mesh):
    return jax.shard_map(
        shards,
        mesh=mesh,
        in_specs=(
            P(None, "mel", "tm"),
            P(),
            P(),
            P(),
            P(),
            P(),
            P(),
            P(),
            P(None, None, "mel", "tm"),
        ),
        out_specs=(P(None, None, "mel", "tm"), P(None, "mel", "tm"), P(), P(), P(), P(), P(), P()),
        check_vma=False,
    )
```

```python
import math

import jax
import jax.numpy as jnp
from jax import lax
from jax.experimental import pallas as pl
from jax.experimental.pallas import tpu as pltpu
from jax.sharding import PartitionSpec as P

F32 = jnp.float32
BF16 = jnp.bfloat16
AXES = ("mel", "tm")
EXACT = lax.Precision.HIGHEST
RIM = 128
BAND = 24
MEL_ROWS = 16
FIRST = 24
SUMS, EDGES, COLUMNS = 16, 19, 23
SIDE = 96
SECOND = 8


def iota(shape, dim):
    return lax.broadcasted_iota(jnp.int32, shape, dim)


def dot(a, b, over=((1,), (0,)), precision=None):
    return lax.dot_general(a, b, (over, ((), ())), precision=precision, preferred_element_type=F32)


def to_column(lanes, count, start=0):
    shape = (count, lanes.shape[1])
    return jnp.sum(jnp.where(iota(shape, 1) == iota(shape, 0) + start, lanes, 0.0), axis=1, keepdims=True)


def to_lanes(column, start=0, width=128):
    shape = (column.shape[0], width)
    return jnp.sum(jnp.where(iota(shape, 1) == iota(shape, 0) + start, column, 0.0), axis=0, keepdims=True)


def halves(v):
    total = v[:, :128]
    for n in range(128, v.shape[1], 128):
        total = total + v[:, n : n + 128]
    return total


def frame_masks(bounds, frames):
    last = bounds.shape[1] - 1

    def living(f):
        return (f >= 0) & (f < bounds[0, last])

    def paired(f):
        both = living(f) & living(f + 1)
        for k in range(1, last):
            both = both & (f + 1 != bounds[0, k])
        return both

    return tuple(m.astype(F32) for m in (living(frames), paired(frames - 1), paired(frames)))


def row_valid(row, rows):
    mel = lax.axis_index("mel") * rows + row
    return ((mel >= 0) & (mel < lax.axis_size("mel") * rows)).astype(F32)


def start_all(*pairs, sems):
    copies = [pltpu.make_async_copy(src, dst, sems.at[n]) for n, (src, dst) in enumerate(pairs)]
    for copy in copies:
        copy.start()
    return copies


def wait_all(copies):
    for copy in copies:
        copy.wait()


def shifted_frames(value, behind, ahead):
    wide = value.shape[1]
    return pltpu.roll(value, 1, 1) * behind, pltpu.roll(value, wide - 1, 1) * ahead


def three_parts(v):
    high = lax.reduce_precision(v, 8, 7)
    mid = lax.reduce_precision(v - high, 8, 7)
    return high, mid, v - high - mid


def share_of(devices, chan):
    return -(-chan // devices)


def pack(spec_hbm, grad_hbm, bounds_hbm, out, own, spec, masks, bounds, edges, rows_out, sems):
    copies = start_all((bounds_hbm, bounds), (spec_hbm, spec), (grad_hbm, own), sems=sems)
    copies[0].wait()
    wide = masks.shape[1]
    frame_dev = wide - RIM
    devices = out.shape[0]
    rows = MEL_ROWS
    lane = iota((1, wide), 1)
    frames = lax.axis_index("tm") * frame_dev + jnp.where(lane < frame_dev + RIM // 2, lane, lane - wide)
    last = bounds.shape[1] - 1
    pixels = (bounds[0, last] * (lax.axis_size("mel") * rows)).astype(F32)
    found = frame_masks(bounds, frames)
    masks[...] = jnp.concatenate(
        list(found) + [jnp.full((1, wide), 1.0) * pixels, jnp.zeros((4, wide), F32)], axis=0
    )
    usable, behind, ahead = (m[:, :frame_dev] for m in found)
    copies[1].wait()
    x = spec[0].astype(F32) * usable
    lane = iota((1, frame_dev), 1)
    row = iota((rows, 1), 0)
    inner = jnp.where((lane > 0) & (lane < frame_dev - 1), usable, 0.0)
    number = (rows - 2) * jnp.sum(inner, axis=1, keepdims=True)
    inner = inner * ((row > 0) & (row < rows - 1)).astype(F32)
    centre = jnp.sum(jnp.sum(x, axis=0, keepdims=True), axis=1, keepdims=True)
    centre = centre / (rows * jnp.maximum(jnp.sum(usable, axis=1, keepdims=True), 1.0))
    centre = lax.reduce_precision(centre, 8, 7)
    shifted = [pltpu.roll(x, 1, 1) * behind, x, pltpu.roll(x, frame_dev - 1, 1) * ahead]
    taps = [pltpu.roll(v, (1 - i) % rows, 0) if i != 1 else v for i in range(3) for v in shifted]
    features = feature_rows(centre, (taps, inner))
    lane = iota((1, 128), 1)
    features = jnp.where(lane == 90, centre, jnp.where(lane == 91, number, features))
    pick = iota((8, frame_dev), 0)
    column = jnp.where(pick < 4, pick, frame_dev - 8 + pick)
    strip = dot((iota((8, frame_dev), 1) == column).astype(BF16), x.astype(BF16), ((1,), (1,)))
    lane = iota((8, 128), 1)
    repeat = (iota((rows, 128), 1) % rows == iota((rows, 128), 0)).astype(BF16)
    strip = jnp.where(lane // rows == iota((8, 128), 0), dot(strip.astype(BF16), repeat), 0.0)
    strip = jnp.sum(strip, axis=0, keepdims=True)

    def put(n, value):
        rows_out[pl.ds(n, devices, stride=FIRST), :] = jnp.broadcast_to(value, (devices, 128))

    near = jnp.concatenate([x[0:4], x[rows - 4 :]], axis=0)
    near = jnp.concatenate([near[:, :128], near[:, 128:]], axis=0)
    for d in range(devices):
        rows_out[FIRST * d : FIRST * d + 16, :] = near
    put(COLUMNS, strip)
    copies[2].wait()
    _, chan, many, half = own.shape
    share = share_of(devices, chan)
    holders = chan // share
    g = own[0].astype(F32)
    edges[0:chan] = g[:, 0, :]
    edges[chan:] = g[:, many - 1, :]

    def spread_out(v):
        if holders < devices:
            v = jnp.concatenate([v, jnp.zeros((devices - holders, 128), F32)], axis=0)
        return v

    for n in range(share):
        put(EDGES + n, spread_out(edges[n * holders : (n + 1) * holders, :]))
        put(EDGES + share + n, spread_out(edges[chan + n * holders : chan + (n + 1) * holders, :]))
    for n in range(2 * share, COLUMNS - EDGES):
        put(EDGES + n, jnp.zeros((1, 128), F32))
    end = iota((8, half), 0)
    at = iota((8, half), 1)
    ends = ((end == 0) & (at == 0)) | ((end == 1) & (at == half - 1))
    columns = dot(ends.astype(BF16), g.reshape(chan * many, half).astype(BF16), ((1,), (1,)))
    group = 128 // many
    source = iota((128, 128), 0)
    lane = iota((group, 128), 1)
    mine = lane // many == iota((group, 128), 0)
    parts = three_parts(features)
    for n in range(2):
        side = jnp.zeros((holders, 128), F32)
        for m in range(share):
            move = (iota((128, 128), 1) == SIDE + many * m + source % many).astype(BF16)
            first = m * holders * many // 128
            block = [columns[n : n + 1, 128 * q : 128 * (q + 1)] for q in range(first, first + holders * many // 128)]
            block = jnp.concatenate([jnp.where(mine, v, 0.0) for v in block], axis=0)
            side = side + dot(block.astype(BF16), move)
        put(SUMS + n, spread_out(side) + parts[n])
    put(SUMS + 2, parts[2])
    out[...] = rows_out[...].reshape(out.shape).astype(BF16)


def weights(own, bounds_hbm, k2_hbm, k1_hbm, gain_one_hbm, bias_one_hbm, gain_two_hbm, bias_two_hbm,
            wf, wb, w1, ws_hbm, pairs, singles, k1t, params, all_masks, edge_masks, twice, own_rows,
            k2, k1, vectors, bounds, ws, temp, sems):
    loads = start_all(
        (bounds_hbm, bounds),
        (k2_hbm, k2),
        (k1_hbm, k1),
        (gain_one_hbm, vectors.at[0]),
        (bias_one_hbm, vectors.at[1]),
        (gain_two_hbm, vectors.at[2]),
        (bias_two_hbm, vectors.at[3]),
        sems=sems,
    )
    _, many, count, half = own.shape
    temp[...] = own[0].astype(F32).reshape(many * count, half)
    for r in range(count):
        own_rows[r * many : (r + 1) * many] = temp[pl.ds(r, many, stride=count), :].astype(BF16)
    wait_all(loads)
    chan = k2.shape[1]
    span = wf.shape[1]
    taps = [k2[t].astype(F32) for t in range(9)]
    rest = jnp.zeros((chan, span - 9 * chan), F32)
    forward = jnp.concatenate(taps + [rest], axis=1)
    backward = jnp.concatenate([taps[8 - t].T for t in range(9)] + [rest], axis=1)
    for r in range(wb.shape[0] // chan):
        at = slice(r * chan, (r + 1) * chan)
        wb[at] = (pltpu.roll(backward, 3 * chan * r, 1) if r else backward).astype(BF16)
    full = jnp.concatenate([k1[n].astype(F32) for n in range(3)] + [jnp.zeros((7, chan), F32)], axis=0)
    low = [
        jnp.concatenate([full[3 * (2 - a) + 2 - b : 3 * (2 - a) + 3 - b] for a in range(3)], axis=1)
        for b in range(3)
    ]
    base = jnp.concatenate(low + [jnp.zeros((5, 3 * chan), F32)], axis=0)
    base = jnp.concatenate([base, jnp.zeros((8, ws.shape[1] - 3 * chan), F32)], axis=1)
    for m in range(ws.shape[0] // 8):
        ws[8 * m : 8 * m + 8] = (pltpu.roll(base, chan * m, 1) if m else base).astype(BF16)
    store_ws = pltpu.make_async_copy(ws, ws_hbm, sems.at[7])
    store_ws.start()
    count, frame_dev = all_masks.shape[0] // 3, all_masks.shape[1]
    frames = iota((count, frame_dev), 0) * frame_dev + iota((count, frame_dev), 1)
    for n, mask in enumerate(frame_masks(bounds, frames)):
        all_masks[n * count : (n + 1) * count] = mask
    q = iota(edge_masks.shape, 0)
    lane = iota(edge_masks.shape, 1)
    k = q % 8
    frames = (q // 8) * frame_dev + jnp.where(k < 4, k, k + frame_dev - 8)
    living, behind, ahead = frame_masks(bounds, frames)
    living = jnp.where((k == 0) | (k == 7), living, 0.0)
    edge_masks[...] = jnp.where(lane == 0, living, jnp.where(lane == 1, behind, jnp.where(lane == 2, ahead, 0.0)))
    params[...] = jnp.concatenate(
        [vectors[n] for n in range(4)] + [jnp.zeros((4, chan), F32)], axis=0
    )
    tap = iota((16, 128), 0)
    lane = iota((16, 128), 1)
    i = (tap * 11) >> 5
    ninth = (lane * 57) >> 9
    to_band = (lane == BAND * (tap - 3 * i) + i) & (tap < 9)
    to_left = (ninth == tap) & (tap < 9)
    to_right = (lane - 9 * ninth == tap) & (lane < 81)
    to_single = (lane == 81 + tap) & (tap < 9)
    source = iota((128, 128), 0) - 81
    lane = iota((128, 128), 1)
    ninth = (lane * 57) >> 9
    inside = (source >= 0) & (source < 9) & (lane < 81)
    twice[...] = jnp.where(inside, (source == ninth).astype(F32) + (source == lane - 9 * ninth).astype(F32), 0.0)
    for r in range(wf.shape[0] // chan):
        at = slice(r * chan, (r + 1) * chan)
        wf[at] = (pltpu.roll(forward, 3 * chan * r, 1) if r else forward).astype(BF16)
    k1t[...] = full
    k = full.astype(BF16)
    lanes = [dot(k, select.astype(BF16), ((0,), (0,))) for select in (to_band, to_left, to_right, to_single)]
    pairs[...] = lanes[1] * lanes[2]
    singles[...] = lanes[3]
    for m in range(w1.shape[0] // chan):
        w1[m * chan : (m + 1) * chan] = (pltpu.roll(lanes[0], m, 1) if m else lanes[0]).astype(BF16)
    store_ws.wait()


def feature_rows(centre, *parts):
    def folded(v):
        return jnp.sum(halves(v), axis=0, keepdims=True)

    rows = [jnp.zeros((1, 128), F32)] * 96
    for taps, weight in parts:
        z = [tap - centre for tap in taps]
        for s in range(9):
            left = z[s] * weight
            rows[81 + s] = rows[81 + s] + folded(left)
            for t in range(s, 9):
                rows[9 * s + t] = rows[9 * t + s] = rows[9 * s + t] + folded(left * z[t])
    return to_lanes(jnp.sum(jnp.concatenate(rows, axis=0), axis=1, keepdims=True))


def summed_blocks(ref, devices):
    block = ref.shape[0] // devices
    period = 8 // math.gcd(block, 8)
    step = period * block
    total = ref[0:step, :]
    for at in range(step, ref.shape[0], step):
        total = total + ref[at : at + step, :]
    result = total[0:block]
    for n in range(1, period):
        result = result + total[n * block : (n + 1) * block]
    return result


def moved_rows(v, step):
    if step == 0:
        return v
    count = v.shape[0]
    if abs(step) >= count:
        return jnp.zeros_like(v)
    zero = jnp.zeros((abs(step), v.shape[1]), v.dtype)
    if step > 0:
        return jnp.concatenate([zero, v[: count - step]], axis=0)
    return jnp.concatenate([v[-step:], zero], axis=0)


def silu_halves(h):
    t = jnp.tanh(h)
    one = 1.0 + t
    return h * one, one * (1.0 + h * (1.0 - t))


def forward_one(recv, spec, pairs, singles, twice, w1, wf, params, masks, all_masks, edge_masks,
                pre_two, payload, act, x3, stats, features_out, pre_one, got, strips, halo, rows_out):
    devices = recv.shape[0]
    n_mel, count = lax.axis_size("mel"), lax.axis_size("tm")
    rows = MEL_ROWS
    mels = n_mel * rows
    wide = masks.shape[1]
    frame_dev = wide - RIM
    chan = params.shape[1]
    me_m, me_t = lax.axis_index("mel"), lax.axis_index("tm")
    usable, behind, ahead = (masks[n : n + 1] for n in range(3))
    total = masks[3:4, 0:1]
    got[...] = recv[...].astype(F32).reshape(devices * FIRST, 128)

    def every(n):
        return got[pl.ds(n, devices, stride=FIRST), :]

    lane = iota((count, 128), 1)
    bands = [got[pl.ds(FIRST * k * count + COLUMNS, count, stride=FIRST), :] for k in range(n_mel)]
    for c in range(8):
        column = jnp.zeros((count, 128), F32)
        for k, band in enumerate(bands):
            part = jnp.where(lane // rows == c, band, 0.0)
            column = column + (pltpu.roll(part, rows * (k - c) % 128, 1) if k != c else part)
        strips[pl.ds(c, count, stride=8), :] = column
    at = pl.multiple_of(FIRST * (jnp.maximum(me_m - 1, 0) * count + me_t), 8)
    above = got[pl.ds(at, 16), :] * (me_m > 0).astype(F32)
    at = pl.multiple_of(FIRST * (jnp.minimum(me_m + 1, n_mel - 1) * count + me_t), 8)
    below = got[pl.ds(at, 16), :] * (me_m < n_mel - 1).astype(F32)
    above = jnp.concatenate([above[4:8], above[12:16]], axis=1)
    below = jnp.concatenate([below[0:4], below[8:12]], axis=1)
    own = spec[0].astype(F32) * usable[:, :frame_dev]
    at = pl.multiple_of(8 * jnp.minimum(me_t + 1, count - 1), 8)
    after = strips[pl.ds(at, 8), :][:, :mels] * (me_t + 1 < count).astype(F32)
    at = pl.multiple_of(8 * jnp.maximum(me_t - 1, 0), 8)
    before = strips[pl.ds(at, 8), :][:, :mels] * (me_t > 0).astype(F32)
    sides = jnp.concatenate([after[0:4], before[4:8], jnp.zeros((8, mels), F32)], axis=0).astype(BF16)
    side = iota((16, RIM), 0)
    place = iota((16, RIM), 1) == jnp.where(side < 4, side, jnp.where(side < 8, side + RIM - 8, -1))
    halo[0:8] = jnp.zeros((8, RIM), F32)
    halo[mels : mels + 8] = jnp.zeros((8, RIM), F32)
    halo[4 : mels + 4] = dot(sides, place.astype(BF16), ((0,), (0,)))
    rim = halo[pl.ds(pl.multiple_of(me_m * rows, 8), BAND), :]
    near = jnp.concatenate([jnp.concatenate([above, own, below], axis=0), rim], axis=1)
    x3[...] = jnp.concatenate(
        [
            pltpu.roll(near, 1, 1) * behind,
            near,
            pltpu.roll(near, wide - 1, 1) * ahead,
            jnp.broadcast_to(usable, (BAND, wide)),
            jnp.zeros((128 - 4 * BAND, wide), F32),
        ],
        axis=0,
    ).astype(BF16)
    pre_one[...] = dot(w1[...], x3[...])
    lane = iota((1, 128), 1)
    parts = jnp.where(lane < 92, every(SUMS) + every(SUMS + 1) + every(SUMS + 2), 0.0)
    centres, numbers = parts[:, 90:91], parts[:, 91:92]
    centre = jnp.sum(centres * numbers, axis=0, keepdims=True)
    centre = centre / jnp.maximum(jnp.sum(numbers, axis=0, keepdims=True), 1.0)
    delta = centres - centre
    features = jnp.sum(parts + delta * numbers * jnp.where(lane < 81, delta, 1.0), axis=0, keepdims=True)
    moved = jnp.sum(delta * parts, axis=0, keepdims=True)
    def edge_row(k, n):
        first = FIRST * k * count + n
        return jnp.concatenate(
            [got[pl.ds(first, count, stride=FIRST), :], got[pl.ds(first + 8, count, stride=FIRST), :]], axis=1
        )

    edge_rows = [[edge_row(k, n) for n in (0, 1, 6, 7)] for k in range(n_mel)]
    zero = jnp.zeros((count, frame_dev), F32)
    rows_of = [[], [], []]
    for k, (top, second, fore, bottom) in enumerate(edge_rows):
        for n, v in enumerate((edge_rows[k - 1][3] if k else zero, top, second)):
            rows_of[n].append(v)
        for n, v in enumerate((fore, bottom, edge_rows[k + 1][0] if k + 1 < n_mel else zero)):
            rows_of[n].append(v)
    f_usable, f_behind, f_ahead = (all_masks[n * count : (n + 1) * count, :] for n in range(3))
    lane = iota((count, frame_dev), 1)

    def frame_before(v):
        v = pltpu.roll(v, 1, 1)
        return jnp.where(lane == 0, pltpu.roll(v, 1, 0), v) * f_behind

    def frame_after(v):
        v = pltpu.roll(v, frame_dev - 1, 1)
        return jnp.where(lane == frame_dev - 1, pltpu.roll(v, count - 1, 0), v) * f_ahead

    taps = []
    for group in rows_of:
        for move in (frame_before, lambda v: v, frame_after):
            taps.append(jnp.concatenate([move(v) for v in group], axis=1))
    f_usable = jnp.concatenate([f_usable] * (2 * n_mel), axis=1)
    borders = (taps, f_usable)
    edge = strips[...]
    q_usable, q_behind, q_ahead = (edge_masks[:, n : n + 1] for n in range(3))
    lane = iota((count * 8, 128), 1)
    inside = (lane < mels) & (lane % rows != 0) & (lane % rows != rows - 1)
    shifted = [
        pltpu.roll(edge, 1, 0) * q_behind,
        edge,
        pltpu.roll(edge, count * 8 - 1, 0) * q_ahead,
    ]
    taps = [pltpu.roll(v, (1 - i) % 128, 1) if i != 1 else v for i in range(3) for v in shifted]
    features = features + feature_rows(centre, borders, (taps, jnp.where(inside, q_usable, 0.0)))
    features = jnp.where(iota((1, 128), 1) < 90, features, 0.0)
    near_mean = jnp.sum(singles[...] * features, axis=1, keepdims=True) / total
    around = jnp.sum(singles[...], axis=1, keepdims=True)
    square = jnp.sum(pairs[...] * features, axis=1, keepdims=True)
    square = (square + 2.0 * around * jnp.sum(singles[...] * moved, axis=1, keepdims=True)) / total
    inv = lax.rsqrt(square - near_mean * near_mean + 1e-05)
    mean = near_mean + centre * around
    lane = iota((chan, 128), 1)
    stats[0:chan] = jnp.where(lane == 0, mean, jnp.where(lane == 1, inv, 0.0))
    stats[chan : chan + 8] = jnp.broadcast_to(to_lanes(near_mean), (8, 128))
    stats[chan + 8 : chan + 16] = jnp.broadcast_to(to_lanes(inv), (8, 128))
    scale = 0.5 * to_column(params[0:1], chan) * inv
    shift = 0.5 * to_column(params[1:2], chan) - mean * scale
    stats[chan + 16 :] = jnp.where(lane == 0, scale, jnp.where(lane == 1, shift, 0.0))
    scale = jnp.broadcast_to(scale, (chan, wide))
    shift = jnp.broadcast_to(shift, (chan, wide))
    ext = w1.shape[0] // chan
    block, taps = wf.shape
    first = jnp.zeros((chan, 128), F32)
    second = jnp.zeros((chan, 128), F32)
    own_mask = usable[:, :frame_dev]
    low_masks = [m.astype(BF16) for m in (usable, behind, ahead)]
    for r in range(ext):
        value, _ = silu_halves(pre_one[r * chan : (r + 1) * chan, :] * scale + shift)
        if not 0 <= r - 3 < rows:
            value = value * row_valid(r - 3, rows)
        base = r * 3 * chan
        low = value.astype(BF16) * low_masks[0]
        act[base : base + chan, :], act[base + 2 * chan : base + 3 * chan, :] = shifted_frames(low, *low_masks[1:])
        act[base + chan : base + 2 * chan, :] = low
        if r < 3 or r % 2 == 0:
            continue
        g = (r - 3) // 2
        result = dot(wf[...], act[g * 3 * block : g * 3 * block + taps, :])
        pre_two[g * block : (g + 1) * block] = result
        for q in range(2):
            if 2 <= 2 * g + q < rows + 2:
                p = result[q * chan : (q + 1) * chan, :frame_dev]
                masked = p * own_mask
                first = first + halves(masked)
                second = second + halves(masked * p)
    moved = dot(jnp.broadcast_to(moved, (8, 128)), twice[...], precision=EXACT)[0:1]
    features_out[...] = jnp.concatenate(
        [features + moved, jnp.broadcast_to(centre, (1, 128)), jnp.zeros((6, 128), F32)], axis=0
    )
    share = share_of(devices, chan)

    def put(n, value):
        rows_out[pl.ds(n, devices, stride=SECOND), :] = jnp.broadcast_to(value, (devices, 128))

    for n in range(share):
        put(3 + n, moved_rows(every(EDGES + share + n), count))
        put(3 + share + n, moved_rows(every(EDGES + n), -count))
    for n in range(3 + 2 * share, SECOND - 1):
        put(n, jnp.zeros((1, 128), F32))
    lane = iota((devices, 128), 1)
    tm = iota((devices, 128), 0) % count
    lefts = jnp.where(lane >= SIDE, every(SUMS), 0.0)
    rights = jnp.where(lane >= SIDE, every(SUMS + 1), 0.0)
    beside = jnp.zeros((devices, 128), F32)
    for n, step in enumerate((0, count, -count)):
        one = jnp.where(tm > 0, moved_rows(rights, step + 1), 0.0)
        two = jnp.where(tm < count - 1, moved_rows(lefts, step - 1), 0.0)
        beside = beside + pltpu.roll(one, (32 * n - SIDE) % 128, 1) + pltpu.roll(two, (32 * n + 16 - SIDE) % 128, 1)
    put(SECOND - 1, beside)
    first = jnp.sum(first, axis=1, keepdims=True)
    second = jnp.sum(second, axis=1, keepdims=True)
    for n, part in enumerate(three_parts(to_lanes(first) + to_lanes(second, chan))):
        put(n, part)
    payload[...] = rows_out[...].reshape(payload.shape).astype(BF16)


def sum_rows(devices, taps):
    return -(-taps // devices) + 2


def backward_scaled(recv, pre_two, act, own_rows, params, masks,
                    grad, payload, pairs, stats, sides, right, got, beyond):
    devices = recv.shape[0]
    got[...] = recv[...].astype(F32).reshape(devices * SECOND, 128)
    chan = params.shape[1]
    half = own_rows.shape[1]
    lane = iota((half, 2 * half), 1)
    spread = jnp.where(lane >> 1 == iota((half, 2 * half), 0), 0.25, 0.0).astype(BF16)
    rows = MEL_ROWS
    wide = pre_two.shape[1]
    frame_dev = wide - RIM
    usable = masks[0:1]
    share = share_of(devices, chan)
    holders = chan // share

    def every(n):
        return got[pl.ds(n, devices, stride=SECOND), :]

    beside = every(SECOND - 1)[:holders]
    lane = iota((holders, RIM), 1)
    many = rows // 2
    for n in range(share):
        first = n * holders
        beyond[first : first + holders, :] = every(3 + n)[:holders]
        beyond[chan + first : chan + first + holders, :] = every(3 + share + n)[:holders]
        for r in range(many + 2):
            at = many * n + (r if r < many else 32 + many - 1 if r == many else 64)
            left, right_of = beside[:, at : at + 1], beside[:, at + 16 : at + 17]
            side = jnp.where(lane >= RIM - 2, 0.25 * left, jnp.where(lane < 2, 0.25 * right_of, 0.0))
            sides[r * chan + first : r * chan + first + holders, :] = side
    total = masks[3:4, 0:1]
    sums = jnp.sum(every(0) + every(1) + every(2), axis=0, keepdims=True)
    mean = to_column(sums, chan) / total
    inv = lax.rsqrt(to_column(sums, chan, chan) / total - mean * mean + 1e-05)
    lane = iota((chan, 128), 1)
    scale = 0.5 * to_column(params[2:3], chan) * inv
    shift = 0.5 * to_column(params[3:4], chan) - mean * scale
    columns = jnp.zeros((chan, 128), F32)
    for n, column in enumerate((mean, inv, scale, shift)):
        columns = jnp.where(lane == n, column, columns)
    stats[0:chan] = columns
    stats[chan : chan + 8] = jnp.broadcast_to(to_lanes(inv), (8, 128))
    shift = jnp.broadcast_to(shift, (chan, wide))
    scale = jnp.broadcast_to(scale, (chan, wide))
    mean = jnp.broadcast_to(mean, (chan, frame_dev))
    inv = jnp.broadcast_to(inv, (chan, frame_dev))
    first = jnp.zeros((chan, 128), F32)
    second = jnp.zeros((chan, 128), F32)
    own_mask = usable[:, :frame_dev]
    right[3 * chan :] = jnp.ones((16, rows * frame_dev), BF16)
    table = jnp.zeros((9 * chan, 3 * chan + 16), F32)
    for q in list(range(2, rows + 2)) + [0, 1, rows + 2, rows + 3]:
        r = q // 2
        at = slice(q * chan, (q + 1) * chan)
        m = q - 2
        mask = 0.5 * usable if 0 <= m < rows else usable * (0.5 * row_valid(m, rows))
        if q % 2 == 0:
            if 1 <= r <= rows // 2:
                pooled, at_side = own_rows[(r - 1) * chan : r * chan], (r - 1) * chan
            elif r == 0:
                pooled, at_side = beyond[0:chan].astype(BF16), many * chan
            else:
                pooled, at_side = beyond[chan:].astype(BF16), (many + 1) * chan
            up = jnp.concatenate([dot(pooled, spread), sides[at_side : at_side + chan, :]], axis=1)
        pre = pre_two[at, :]
        value, slope = silu_halves(pre * scale + shift)
        g = up * slope * mask
        grad[at, :] = g
        if not 0 <= m < rows:
            continue
        g = g[:, :frame_dev]
        normed = (pre[:, :frame_dev] - mean) * inv
        first = first + halves(g * normed)
        second = second + halves(g)
        value = value[:, :frame_dev] * own_mask
        both = value if m % 2 == 0 else both + value
        if m % 2:
            pairs[(r - 1) * chan : r * chan, :] = both
        lanes = slice(m * frame_dev, (m + 1) * frame_dev)
        high = lax.reduce_precision(g, 8, 7)
        right[0:chan, lanes] = high.astype(BF16)
        right[chan : 2 * chan, lanes] = (g - high).astype(BF16)
        right[2 * chan : 3 * chan, lanes] = normed.astype(BF16)
        if m % 4 == 3:
            left = [act[(n + 2) * 3 * chan : (n + 5) * 3 * chan, :frame_dev] for n in range(m - 3, m + 1)]
            lanes = slice((m - 3) * frame_dev, (m + 1) * frame_dev)
            table = table + dot(jnp.concatenate(left, axis=1), right[:, lanes], ((1,), (1,)))
    first = jnp.sum(first, axis=1, keepdims=True)
    second = jnp.sum(second, axis=1, keepdims=True)
    totals = to_lanes(first) + to_lanes(second, chan)
    block = payload.shape[0] // devices
    payload[pl.ds(0, devices, stride=block), :] = jnp.broadcast_to(totals, (devices, 128))
    both = jnp.concatenate([table[:, :chan] + table[:, chan : 2 * chan], table[:, 2 * chan : 3 * chan]], axis=1)
    single = table[:, 3 * chan : 3 * chan + 1]
    lane = iota((devices, 128), 1)
    constants = jnp.zeros((devices, 128), F32)
    for k in range(block - 2):
        cut, ones = both[k * devices : (k + 1) * devices], single[k * devices : (k + 1) * devices]
        short = devices - cut.shape[0]
        if short:
            cut = jnp.concatenate([cut, jnp.zeros((short, 128), F32)], axis=0)
            ones = jnp.concatenate([ones, jnp.zeros((short, 1), F32)], axis=0)
        payload[pl.ds(1 + k, devices, stride=block), :] = cut
        constants = jnp.where(lane == k, ones, constants)
    payload[pl.ds(block - 1, devices, stride=block), :] = constants


def pool(totals, pairs, out, gain_out, bias_out, temp):
    gain_out[...] = totals[0:1, : gain_out.shape[1]]
    bias_out[...] = totals[0:1, gain_out.shape[1] :]
    chan, rows, half = out.shape[1:]
    to_mean = jnp.where(iota((2 * half, half), 0) >> 1 == iota((2 * half, half), 1), 0.25, 0.0)
    pooled = dot(pairs[...], to_mean, precision=EXACT)
    for r in range(rows):
        temp[pl.ds(r, chan, stride=rows), :] = pooled[r * chan : (r + 1) * chan]
    out[0] = temp[...].reshape(chan, rows, half).astype(BF16)


def backward(recv, pre_two, grad, stats_two, w1, x3, stats, params, masks, wb,
             out, payload, totals, g3, pre_one, g1):
    chan = params.shape[1]
    rows = MEL_ROWS
    wide = pre_two.shape[1]
    frame_dev = wide - RIM
    usable = masks[0:1]
    behind, ahead = (masks[n : n + 1].astype(BF16) for n in (1, 2))
    total = masks[3:4, 0:1]
    devices = payload.shape[0] // 14
    pre_one[...] = dot(w1[2 * chan : (rows + 4) * chan], x3[...])

    received = summed_blocks(recv, devices)
    sums = received[0:1]
    gain_sum, bias_sum = sums[:, :chan], sums[:, chan:]
    totals[...] = jnp.broadcast_to(sums, (8, 128))
    mean, inv = stats_two[0:chan, 0:1], stats_two[0:chan, 1:2]
    factor = to_column(params[2:3], chan) * inv
    gain_part = factor * (to_column(sums, chan) / total * inv)
    bias_part = factor * (to_column(sums, chan, chan) / total) - mean * gain_part
    gain_part = jnp.broadcast_to(gain_part, (chan, wide))
    bias_part = jnp.broadcast_to(bias_part, (chan, wide))
    factor = jnp.broadcast_to(factor, (chan, wide))
    scale = jnp.broadcast_to(stats[chan + 16 :, 0:1], (chan, wide))
    shift = jnp.broadcast_to(stats[chan + 16 :, 1:2], (chan, wide))
    factor_one = jnp.broadcast_to(to_column(params[0:1], chan) * stats[0:chan, 1:2], (chan, wide))
    count = pre_two.shape[0] // chan
    table = jnp.zeros((chan, 128), F32)
    for q in range(count):
        at = slice(q * chan, (q + 1) * chan)
        mask = usable if 0 <= q - 2 < rows else usable * row_valid(q - 2, rows)
        low = (factor * grad[at, :] - (bias_part + pre_two[at, :] * gain_part) * mask).astype(BF16)
        base = q * 3 * chan
        g3[base : base + chan, :], g3[base + 2 * chan : base + 3 * chan, :] = shifted_frames(low, behind, ahead)
        g3[base + chan : base + 2 * chan, :] = low
        if q < 3 or q % 2 == 0:
            continue
        start = q - 3
        result = dot(wb[...], g3[start * 3 * chan : (start + 4) * 3 * chan, :])
        for n in range(2):
            m = start + n - 1
            at = slice((m + 1) * chan, (m + 2) * chan)
            _, slope = silu_halves(pre_one[at, :] * scale + shift)
            mask = 0.5 * usable if 0 <= m < rows else usable * (0.5 * row_valid(m, rows))
            value = result[n * chan : (n + 1) * chan] * slope * mask
            out[at, :] = (value * factor_one).astype(BF16)
            if not 0 <= m < rows:
                continue
            g1[m * chan : (m + 1) * chan, :] = value[:, :frame_dev]
            if m % 4 == 3:
                part = g1[(m - 3) * chan : (m + 1) * chan, :]
                high = lax.reduce_precision(part, 8, 7)
                low = (part - high).astype(BF16)
                taps_in = x3[:, :frame_dev]
                products = dot(high.astype(BF16), taps_in, ((1,), (1,))) + dot(low, taps_in, ((1,), (1,)))
                for k in range(4):
                    table = table + pltpu.roll(products[k * chan : (k + 1) * chan], 128 - (m + k), 1)
    tap = iota((16, 128), 0)
    lane = iota((16, 128), 1)
    i = (tap * 11) >> 5
    select = ((lane == BAND * (tap - 3 * i) + i) & (tap < 9)) | ((lane == 3 * BAND) & (tap == 9))
    rows10 = dot(select.astype(F32), table, ((1,), (1,)), EXACT)
    share = received.shape[0] - 2
    mine = received[1 : share + 1]
    single = to_column(received[share + 1 :], share)
    factor_l = params[2:3] * stats_two[chan : chan + 1, :chan]
    mine = mine[:, :chan] - (bias_sum * single + gain_sum * mine[:, chan:]) / total
    mine = factor_l * mine
    lower = -(-share // 2)
    mine = jnp.concatenate([mine] + [jnp.zeros((2 * lower - share, chan), F32)] * (share % 2), axis=0)
    mine = jnp.concatenate([mine[:lower], mine[lower:]], axis=1)
    if lower < 9:
        mine = jnp.concatenate([mine, jnp.zeros((9 - lower, 128), F32)], axis=0)
    sums = jnp.concatenate([rows10[0:5], rows10[5:10]], axis=1)
    block = jnp.concatenate([sums, mine], axis=0)
    block = jnp.concatenate([block] * 4, axis=0)
    for d in range(0, devices, 4):
        payload[14 * d : 14 * (d + 4), :] = block


def transposed(low, w1, x3, stats, masks, ws_hbm, first, normed, ws, pre_one, sem):
    load = pltpu.make_async_copy(ws_hbm, ws, sem)
    load.start()
    chan = low.shape[0] // (MEL_ROWS + 2)
    wide = low.shape[1]
    pre_one[...] = dot(w1[2 * chan : (MEL_ROWS + 4) * chan], x3[...])
    mean = jnp.broadcast_to(stats[0:chan, 0:1], (chan, wide))
    inv = jnp.broadcast_to(stats[0:chan, 1:2], (chan, wide))
    for q in range(MEL_ROWS + 2):
        at = slice(q * chan, (q + 1) * chan)
        mask = masks[0:1] * row_valid(q - 1, MEL_ROWS)
        normed[at, :] = ((pre_one[at, :] - mean) * inv * mask).astype(BF16)
    load.wait()
    first[...] = dot(ws[...], low[...])


def finish(recv, features, stats, k1t, first, normed, ws, params, masks,
           spec_hbm, kernel_one_hbm, kernel_two_hbm, gain_hbm, bias_hbm,
           table, spec_grad, kernel_one, kernel_two, gain_out, bias_out, sems):
    chan = params.shape[1]
    rows = MEL_ROWS
    wide = normed.shape[1]
    frame_dev = wide - RIM
    usable, behind, ahead = (masks[n : n + 1] for n in range(3))
    total = masks[3:4, 0:1]
    gain = params[0:1]
    count = recv.shape[0] // 14
    share = -(-9 * chan // count)
    lower = -(-share // 2)
    left = [recv[pl.ds(5 + p, count, stride=14), :] for p in range(lower)]
    whole = jnp.concatenate([v[:, :chan] for v in left] + [v[:, chan:] for v in left], axis=0)
    for t in range(9):
        kernel_two[t] = whole[t * chan : (t + 1) * chan].T
    stores = [pltpu.make_async_copy(kernel_two, kernel_two_hbm, sems.at[3])]
    stores[0].start()
    sums = summed_blocks(recv, count)[0:5]
    ten = jnp.concatenate([sums[:, :chan], sums[:, chan:]], axis=0)
    bias_sum = ten[9:10]
    mean_l, inv_l = stats[chan : chan + 1, :chan], stats[chan + 8 : chan + 9, :chan]
    ten = ten - features[1:2, 0:1] * bias_sum
    k = k1t[0:9]
    gain_sum = inv_l * (jnp.sum(k * ten[0:9], axis=0, keepdims=True) - mean_l * bias_sum)
    gain_out[...] = gain_sum
    bias_out[...] = bias_sum
    for n, (source, target) in enumerate(((gain_out, gain_hbm), (bias_out, bias_hbm))):
        stores.append(pltpu.make_async_copy(source, target, sems.at[n]))
        stores[-1].start()
    factor_l = gain * inv_l
    scale = factor_l * gain_sum / total
    scale = jnp.concatenate([scale, scale], axis=1)
    scale = jnp.concatenate([scale] * ((rows + 2) // 2), axis=1)
    taps = first[...] - dot((ws[...].astype(F32) * scale).astype(BF16), normed[...])
    for part in range(wide // 128):
        table[part] = taps[:, 128 * part : 128 * (part + 1)]
    moved = [
        jnp.concatenate([table[part, pl.ds(b, rows, stride=8), :] for part in range(wide // 128)], axis=1)
        for b in range(3)
    ]
    constant = jnp.sum(k * (factor_l * bias_sum / total), axis=1, keepdims=True)
    for a in range(3):
        row = iota((rows, 1), 0) + (a - 1) + lax.axis_index("mel") * rows
        valid = ((row >= 0) & (row < lax.axis_size("mel") * rows)).astype(F32) * usable
        for b in range(3):
            t = 3 * (2 - a) + 2 - b
            moved[b] = moved[b] - constant[t : t + 1] * valid
    result = pltpu.roll(moved[0], 1, 1) * behind + moved[1] + pltpu.roll(moved[2], wide - 1, 1) * ahead
    spec_grad[0] = (result * usable)[:, :frame_dev]
    stores.append(pltpu.make_async_copy(spec_grad, spec_hbm, sems.at[2]))
    stores[-1].start()
    row = features[0:1, :]
    lane = iota((1, 128), 1)
    gram = jnp.concatenate(
        [jnp.where(lane < 9, pltpu.roll(row, 128 - 9 * t, 1) if t else row, 0.0) for t in range(9)]
        + [jnp.zeros((7, 128), F32)],
        axis=0,
    )
    single = to_column(row, 16, 81)[0:9]
    k_rows = jnp.concatenate([k1t[...], jnp.zeros((112, chan), F32)], axis=0)
    normed_taps = inv_l * (dot(gram, k_rows, precision=EXACT)[0:9] - single * mean_l)
    grad_taps = factor_l * (ten[0:9] - (bias_sum * single + gain_sum * normed_taps) / total)
    for i in range(3):
        kernel_one[i] = grad_taps[3 * i : 3 * i + 3]
    stores.append(pltpu.make_async_copy(kernel_one, kernel_one_hbm, sems.at[4]))
    stores[-1].start()
    for store in stores:
        store.wait()


def run(kernel, outs, scratch, *args, hbm=0, apart=(), flops=10**8, size=4 * 10**6):
    vmem = pl.BlockSpec(memory_space=pltpu.VMEM)
    devices = lax.axis_size("mel") * lax.axis_size("tm")
    specs = []
    args = list(args)
    for n, a in enumerate(args):
        if hbm and n >= len(args) - hbm:
            specs.append(pl.BlockSpec(memory_space=pltpu.HBM))
            args[n] = pltpu.with_memory_space_constraint(a, pltpu.HBM)
        else:
            specs.append(vmem)
            args[n] = pltpu.with_memory_space_constraint(a, pltpu.VMEM)
    return pl.pallas_call(
        kernel,
        out_shape=outs,
        in_specs=specs,
        out_specs=[pl.BlockSpec(memory_space=pltpu.HBM) if n in apart else vmem for n in range(len(outs))],
        scratch_shapes=scratch,
        compiler_params=pltpu.CompilerParams(vmem_limit_bytes=(29 + devices // 32) * 2**20),
        cost_estimate=pl.CostEstimate(flops=flops, bytes_accessed=size, transcendentals=0),
    )(*args)


def shape(dims, dtype=F32):
    return jax.ShapeDtypeStruct(dims, dtype)


def kept(dims, dtype=F32):
    return pltpu.VMEM(dims, dtype)


def far(dims, dtype=F32):
    return pltpu.HBM(dims, dtype)


def exchange(blocks, axes=AXES):
    return lax.all_to_all(blocks, axes, 0, 0, tiled=True)


def exchange_rows(rows, axes=AXES):
    return exchange(rows[:, None, :], axes)[:, 0, :]


def shards(spectrum, clip_bounds, kernel_one, gain_one, bias_one, kernel_two, gain_two, bias_two, pooled_grad):
    _, rows, frame_dev = spectrum.shape
    chan = kernel_two.shape[0]
    n_mel, n_tm = lax.axis_size("mel"), lax.axis_size("tm")
    devices = n_mel * n_tm
    half = frame_dev // 2
    wide = frame_dev + RIM
    mels = n_mel * rows

    packed, own, spec, masks = run(
        pack,
        [
            kept((devices, FIRST, 128), BF16),
            kept(pooled_grad.shape, BF16),
            kept(spectrum.shape, BF16),
            kept((8, wide)),
        ],
        [
            pltpu.SMEM(clip_bounds.shape, jnp.int32),
            pltpu.VMEM((2 * chan, half), F32),
            pltpu.VMEM((devices * FIRST, 128), F32),
            pltpu.SemaphoreType.DMA((3,)),
        ],
        spectrum,
        pooled_grad,
        clip_bounds,
        hbm=3,
    )
    recv = exchange(packed)
    ext = rows + 6
    span = 4 * 3 * chan
    wf, wb, w1, ws, pairs, singles, k1t, params, all_masks, edge_masks, twice, own_rows = run(
        weights,
        [
            kept((2 * chan, span), BF16),
            kept((2 * chan, span), BF16),
            kept((ext * chan, 128), BF16),
            far((rows * 8, (rows + 2) * chan), BF16),
            kept((chan, 128)),
            kept((chan, 128)),
            kept((16, chan)),
            kept((8, chan)),
            kept((3 * n_tm, frame_dev)),
            kept((n_tm * 8, 128)),
            kept((128, 128)),
            kept((chan * rows // 2, half), BF16),
        ],
        [
            pltpu.VMEM((9, chan, chan), BF16),
            pltpu.VMEM((3, 3, chan), BF16),
            pltpu.VMEM((4, 1, chan), F32),
            pltpu.SMEM(clip_bounds.shape, jnp.int32),
            pltpu.VMEM((rows * 8, (rows + 2) * chan), BF16),
            pltpu.VMEM((chan * rows // 2, half), F32),
            pltpu.SemaphoreType.DMA((8,)),
        ],
        own,
        clip_bounds,
        jnp.transpose(kernel_two, (2, 3, 0, 1)).reshape(9, chan, chan),
        jnp.transpose(kernel_one, (1, 2, 0)),
        gain_one[None],
        bias_one[None],
        gain_two[None],
        bias_two[None],
        hbm=7,
        apart=(3,),
    )
    pre_two, payload, act, x3, stats_one, features = run(
        forward_one,
        [
            kept(((rows + 4) * chan, wide)),
            kept((devices, SECOND, 128), BF16),
            kept((ext * 3 * chan, wide), BF16),
            kept((128, wide), BF16),
            kept((2 * chan + 16, 128)),
            kept((8, 128)),
        ],
        [
            pltpu.VMEM((ext * chan, wide), F32),
            pltpu.VMEM((devices * FIRST, 128), F32),
            pltpu.VMEM((n_tm * 8, 128), F32),
            pltpu.VMEM((mels + 8, RIM), F32),
            pltpu.VMEM((devices * SECOND, 128), F32),
        ],
        recv,
        spec,
        pairs,
        singles,
        twice,
        w1,
        wf,
        params,
        masks,
        all_masks,
        edge_masks,
    )
    recv = exchange(payload)
    grad, payload, row_pairs, stats_two = run(
        backward_scaled,
        [
            kept(((rows + 4) * chan, wide)),
            kept((devices * sum_rows(devices, 9 * chan), 128)),
            kept((rows // 2 * chan, frame_dev)),
            kept((chan + 8, 128)),
        ],
        [
            pltpu.VMEM(((rows // 2 + 2) * chan, RIM), F32),
            pltpu.VMEM((3 * chan + 16, rows * frame_dev), BF16),
            pltpu.VMEM((devices * SECOND, 128), F32),
            pltpu.VMEM((2 * chan, half), F32),
        ],
        recv,
        pre_two,
        act,
        own_rows,
        params,
        masks,
    )
    recv = exchange_rows(payload)
    low, payload, totals = run(
        backward,
        [
            kept(((rows + 2) * chan, wide), BF16),
            kept((devices * 14, 128)),
            kept((8, 128)),
        ],
        [
            pltpu.VMEM(((rows + 4) * 3 * chan, wide), BF16),
            pltpu.VMEM(((rows + 2) * chan, wide), F32),
            pltpu.VMEM((rows * chan, frame_dev), F32),
        ],
        recv,
        pre_two,
        grad,
        stats_two,
        w1,
        x3,
        stats_one,
        params,
        masks,
        wb,
    )
    recv = exchange_rows(payload)
    pooled, gain_two_grad, bias_two_grad = run(
        pool,
        [shape((1, chan, rows // 2, half), BF16), shape((1, chan)), shape((1, chan))],
        [
            pltpu.VMEM((rows // 2 * chan, 128), F32),
        ],
        totals,
        row_pairs,
    )
    first, normed, ws = run(
        transposed,
        [
            kept((rows * 8, wide)),
            kept(((rows + 2) * chan, wide), BF16),
            kept((rows * 8, (rows + 2) * chan), BF16),
        ],
        [pltpu.VMEM(((rows + 2) * chan, wide), F32), pltpu.SemaphoreType.DMA],
        low,
        w1,
        x3,
        stats_one,
        masks,
        ws,
        hbm=1,
    )
    spec_grad, kernel_one_grad, kernel_two_grad, gain_one_grad, bias_one_grad = run(
        finish,
        [
            shape((1, rows, frame_dev)),
            shape((3, 3, chan)),
            shape((9, chan, chan)),
            shape((1, chan)),
            shape((1, chan)),
        ],
        [
            pltpu.VMEM((3, rows * 8, 128), F32),
            pltpu.VMEM((1, rows, frame_dev), F32),
            pltpu.VMEM((3, 3, chan), F32),
            pltpu.VMEM((9, chan, chan), F32),
            pltpu.VMEM((1, chan), F32),
            pltpu.VMEM((1, chan), F32),
            pltpu.SemaphoreType.DMA((5,)),
        ],
        recv,
        features,
        stats_one,
        k1t,
        first,
        normed,
        ws,
        params,
        masks,
        apart=range(5),
    )
    kernel_two_grad = jnp.transpose(kernel_two_grad.reshape(3, 3, chan, chan), (2, 3, 0, 1))
    return (
        pooled,
        spec_grad,
        jnp.transpose(kernel_one_grad, (2, 0, 1)),
        gain_one_grad[0],
        bias_one_grad[0],
        kernel_two_grad,
        gain_two_grad[0],
        bias_two_grad[0],
    )


def solution(mesh):
    return jax.shard_map(
        shards,
        mesh=mesh,
        in_specs=(
            P(None, "mel", "tm"),
            P(),
            P(),
            P(),
            P(),
            P(),
            P(),
            P(),
            P(None, None, "mel", "tm"),
        ),
        out_specs=(P(None, None, "mel", "tm"), P(None, "mel", "tm"), P(), P(), P(), P(), P(), P()),
        check_vma=False,
    )
```

```python
import math

import jax
import jax.numpy as jnp
from jax import lax
from jax.experimental import pallas as pl
from jax.experimental.pallas import tpu as pltpu
from jax.sharding import PartitionSpec as P

F32 = jnp.float32
BF16 = jnp.bfloat16
AXES = ("mel", "tm")
EXACT = lax.Precision.HIGHEST
RIM = 128
BAND = 24
MEL_ROWS = 16
FIRST = 24
SUMS, EDGES, COLUMNS = 16, 19, 23
SIDE = 96
SECOND = 8


def iota(shape, dim):
    return lax.broadcasted_iota(jnp.int32, shape, dim)


def dot(a, b, over=((1,), (0,)), precision=None):
    return lax.dot_general(a, b, (over, ((), ())), precision=precision, preferred_element_type=F32)


def to_column(lanes, count, start=0):
    shape = (count, lanes.shape[1])
    return jnp.sum(jnp.where(iota(shape, 1) == iota(shape, 0) + start, lanes, 0.0), axis=1, keepdims=True)


def to_lanes(column, start=0, width=128):
    shape = (column.shape[0], width)
    return jnp.sum(jnp.where(iota(shape, 1) == iota(shape, 0) + start, column, 0.0), axis=0, keepdims=True)


def halves(v):
    total = v[:, :128]
    for n in range(128, v.shape[1], 128):
        total = total + v[:, n : n + 128]
    return total


def frame_masks(bounds, frames):
    last = bounds.shape[1] - 1

    def living(f):
        return (f >= 0) & (f < bounds[0, last])

    def paired(f):
        both = living(f) & living(f + 1)
        for k in range(1, last):
            both = both & (f + 1 != bounds[0, k])
        return both

    return tuple(m.astype(F32) for m in (living(frames), paired(frames - 1), paired(frames)))


def row_valid(row, rows):
    mel = lax.axis_index("mel") * rows + row
    return ((mel >= 0) & (mel < lax.axis_size("mel") * rows)).astype(F32)


def start_all(*pairs, sems):
    copies = [pltpu.make_async_copy(src, dst, sems.at[n]) for n, (src, dst) in enumerate(pairs)]
    for copy in copies:
        copy.start()
    return copies


def wait_all(copies):
    for copy in copies:
        copy.wait()


def shifted_frames(value, behind, ahead):
    wide = value.shape[1]
    return pltpu.roll(value, 1, 1) * behind, pltpu.roll(value, wide - 1, 1) * ahead


def three_parts(v):
    high = lax.reduce_precision(v, 8, 7)
    mid = lax.reduce_precision(v - high, 8, 7)
    return high, mid, v - high - mid


def share_of(devices, chan):
    return -(-chan // devices)


def pack(spec_hbm, grad_hbm, bounds_hbm, out, own, spec, masks, bounds, edges, rows_out, sems):
    copies = start_all((bounds_hbm, bounds), (spec_hbm, spec), (grad_hbm, own), sems=sems)
    copies[0].wait()
    wide = masks.shape[1]
    frame_dev = wide - RIM
    devices = out.shape[0]
    rows = MEL_ROWS
    lane = iota((1, wide), 1)
    frames = lax.axis_index("tm") * frame_dev + jnp.where(lane < frame_dev + RIM // 2, lane, lane - wide)
    last = bounds.shape[1] - 1
    pixels = (bounds[0, last] * (lax.axis_size("mel") * rows)).astype(F32)
    found = frame_masks(bounds, frames)
    masks[...] = jnp.concatenate(
        list(found) + [jnp.full((1, wide), 1.0) * pixels, jnp.zeros((4, wide), F32)], axis=0
    )
    usable, behind, ahead = (m[:, :frame_dev] for m in found)
    copies[1].wait()
    x = spec[0].astype(F32) * usable
    lane = iota((1, frame_dev), 1)
    row = iota((rows, 1), 0)
    inner = jnp.where((lane > 0) & (lane < frame_dev - 1), usable, 0.0)
    number = (rows - 2) * jnp.sum(inner, axis=1, keepdims=True)
    inner = inner * ((row > 0) & (row < rows - 1)).astype(F32)
    centre = jnp.sum(jnp.sum(x, axis=0, keepdims=True), axis=1, keepdims=True)
    centre = centre / (rows * jnp.maximum(jnp.sum(usable, axis=1, keepdims=True), 1.0))
    centre = lax.reduce_precision(centre, 8, 7)
    shifted = [pltpu.roll(x, 1, 1) * behind, x, pltpu.roll(x, frame_dev - 1, 1) * ahead]
    taps = [pltpu.roll(v, (1 - i) % rows, 0) if i != 1 else v for i in range(3) for v in shifted]
    features = feature_rows(centre, (taps, inner))
    lane = iota((1, 128), 1)
    features = jnp.where(lane == 90, centre, jnp.where(lane == 91, number, features))
    pick = iota((8, frame_dev), 0)
    column = jnp.where(pick < 4, pick, frame_dev - 8 + pick)
    strip = dot((iota((8, frame_dev), 1) == column).astype(BF16), x.astype(BF16), ((1,), (1,)))
    lane = iota((8, 128), 1)
    repeat = (iota((rows, 128), 1) % rows == iota((rows, 128), 0)).astype(BF16)
    strip = jnp.where(lane // rows == iota((8, 128), 0), dot(strip.astype(BF16), repeat), 0.0)
    strip = jnp.sum(strip, axis=0, keepdims=True)

    def put(n, value):
        rows_out[pl.ds(n, devices, stride=FIRST), :] = jnp.broadcast_to(value, (devices, 128))

    near = jnp.concatenate([x[0:4], x[rows - 4 :]], axis=0)
    near = jnp.concatenate([near[:, :128], near[:, 128:]], axis=0)
    for d in range(devices):
        rows_out[FIRST * d : FIRST * d + 16, :] = near
    put(COLUMNS, strip)
    copies[2].wait()
    _, chan, many, half = own.shape
    share = share_of(devices, chan)
    holders = chan // share
    g = own[0].astype(F32)
    edges[0:chan] = g[:, 0, :]
    edges[chan:] = g[:, many - 1, :]

    def spread_out(v):
        if holders < devices:
            v = jnp.concatenate([v, jnp.zeros((devices - holders, 128), F32)], axis=0)
        return v

    for n in range(share):
        put(EDGES + n, spread_out(edges[n * holders : (n + 1) * holders, :]))
        put(EDGES + share + n, spread_out(edges[chan + n * holders : chan + (n + 1) * holders, :]))
    for n in range(2 * share, COLUMNS - EDGES):
        put(EDGES + n, jnp.zeros((1, 128), F32))
    end = iota((8, half), 0)
    at = iota((8, half), 1)
    ends = ((end == 0) & (at == 0)) | ((end == 1) & (at == half - 1))
    columns = dot(ends.astype(BF16), g.reshape(chan * many, half).astype(BF16), ((1,), (1,)))
    group = 128 // many
    source = iota((128, 128), 0)
    lane = iota((group, 128), 1)
    mine = lane // many == iota((group, 128), 0)
    parts = three_parts(features)
    for n in range(2):
        side = jnp.zeros((holders, 128), F32)
        for m in range(share):
            move = (iota((128, 128), 1) == SIDE + many * m + source % many).astype(BF16)
            first = m * holders * many // 128
            block = [columns[n : n + 1, 128 * q : 128 * (q + 1)] for q in range(first, first + holders * many // 128)]
            block = jnp.concatenate([jnp.where(mine, v, 0.0) for v in block], axis=0)
            side = side + dot(block.astype(BF16), move)
        put(SUMS + n, spread_out(side) + parts[n])
    put(SUMS + 2, parts[2])
    out[...] = rows_out[...].reshape(out.shape).astype(BF16)


def weights(own, bounds_hbm, k2_hbm, k1_hbm, gain_one_hbm, bias_one_hbm, gain_two_hbm, bias_two_hbm,
            wf, wb, w1, ws_hbm, pairs, singles, k1t, params, all_masks, edge_masks, twice, own_rows,
            k2, k1, vectors, bounds, ws, temp, sems):
    loads = start_all(
        (bounds_hbm, bounds),
        (k2_hbm, k2),
        (k1_hbm, k1),
        (gain_one_hbm, vectors.at[0]),
        (bias_one_hbm, vectors.at[1]),
        (gain_two_hbm, vectors.at[2]),
        (bias_two_hbm, vectors.at[3]),
        sems=sems,
    )
    _, many, count, half = own.shape
    temp[...] = own[0].astype(F32).reshape(many * count, half)
    for r in range(count):
        own_rows[r * many : (r + 1) * many] = temp[pl.ds(r, many, stride=count), :].astype(BF16)
    wait_all(loads)
    chan = k2.shape[1]
    span = wf.shape[1]
    taps = [k2[t].astype(F32) for t in range(9)]
    rest = jnp.zeros((chan, span - 9 * chan), F32)
    forward = jnp.concatenate(taps + [rest], axis=1)
    backward = jnp.concatenate([taps[8 - t].T for t in range(9)] + [rest], axis=1)
    for r in range(wb.shape[0] // chan):
        at = slice(r * chan, (r + 1) * chan)
        wb[at] = (pltpu.roll(backward, 3 * chan * r, 1) if r else backward).astype(BF16)
    full = jnp.concatenate([k1[n].astype(F32) for n in range(3)] + [jnp.zeros((7, chan), F32)], axis=0)
    low = [
        jnp.concatenate([full[3 * (2 - a) + 2 - b : 3 * (2 - a) + 3 - b] for a in range(3)], axis=1)
        for b in range(3)
    ]
    base = jnp.concatenate(low + [jnp.zeros((5, 3 * chan), F32)], axis=0)
    base = jnp.concatenate([base, jnp.zeros((8, ws.shape[1] - 3 * chan), F32)], axis=1)
    for m in range(ws.shape[0] // 8):
        ws[8 * m : 8 * m + 8] = (pltpu.roll(base, chan * m, 1) if m else base).astype(BF16)
    store_ws = pltpu.make_async_copy(ws, ws_hbm, sems.at[7])
    store_ws.start()
    count, frame_dev = all_masks.shape[0] // 3, all_masks.shape[1]
    frames = iota((count, frame_dev), 0) * frame_dev + iota((count, frame_dev), 1)
    for n, mask in enumerate(frame_masks(bounds, frames)):
        all_masks[n * count : (n + 1) * count] = mask
    q = iota(edge_masks.shape, 0)
    lane = iota(edge_masks.shape, 1)
    k = q % 8
    frames = (q // 8) * frame_dev + jnp.where(k < 4, k, k + frame_dev - 8)
    living, behind, ahead = frame_masks(bounds, frames)
    living = jnp.where((k == 0) | (k == 7), living, 0.0)
    edge_masks[...] = jnp.where(lane == 0, living, jnp.where(lane == 1, behind, jnp.where(lane == 2, ahead, 0.0)))
    params[...] = jnp.concatenate(
        [vectors[n] for n in range(4)] + [jnp.zeros((4, chan), F32)], axis=0
    )
    tap = iota((16, 128), 0)
    lane = iota((16, 128), 1)
    i = (tap * 11) >> 5
    ninth = (lane * 57) >> 9
    to_band = (lane == BAND * (tap - 3 * i) + i) & (tap < 9)
    to_left = (ninth == tap) & (tap < 9)
    to_right = (lane - 9 * ninth == tap) & (lane < 81)
    to_single = (lane == 81 + tap) & (tap < 9)
    source = iota((128, 128), 0) - 81
    lane = iota((128, 128), 1)
    ninth = (lane * 57) >> 9
    inside = (source >= 0) & (source < 9) & (lane < 81)
    twice[...] = jnp.where(inside, (source == ninth).astype(F32) + (source == lane - 9 * ninth).astype(F32), 0.0)
    for r in range(wf.shape[0] // chan):
        at = slice(r * chan, (r + 1) * chan)
        wf[at] = (pltpu.roll(forward, 3 * chan * r, 1) if r else forward).astype(BF16)
    k1t[...] = full
    k = full.astype(BF16)
    lanes = [dot(k, select.astype(BF16), ((0,), (0,))) for select in (to_band, to_left, to_right, to_single)]
    pairs[...] = lanes[1] * lanes[2]
    singles[...] = lanes[3]
    for m in range(w1.shape[0] // chan):
        w1[m * chan : (m + 1) * chan] = (pltpu.roll(lanes[0], m, 1) if m else lanes[0]).astype(BF16)
    store_ws.wait()


def feature_rows(centre, *parts):
    def folded(v):
        return jnp.sum(halves(v), axis=0, keepdims=True)

    rows = [jnp.zeros((1, 128), F32)] * 96
    for taps, weight in parts:
        z = [tap - centre for tap in taps]
        for s in range(9):
            left = z[s] * weight
            rows[81 + s] = rows[81 + s] + folded(left)
            for t in range(s, 9):
                rows[9 * s + t] = rows[9 * t + s] = rows[9 * s + t] + folded(left * z[t])
    return to_lanes(jnp.sum(jnp.concatenate(rows, axis=0), axis=1, keepdims=True))


def summed_blocks(ref, devices):
    block = ref.shape[0] // devices
    period = 8 // math.gcd(block, 8)
    step = period * block
    total = ref[0:step, :]
    for at in range(step, ref.shape[0], step):
        total = total + ref[at : at + step, :]
    result = total[0:block]
    for n in range(1, period):
        result = result + total[n * block : (n + 1) * block]
    return result


def moved_rows(v, step):
    if step == 0:
        return v
    count = v.shape[0]
    if abs(step) >= count:
        return jnp.zeros_like(v)
    zero = jnp.zeros((abs(step), v.shape[1]), v.dtype)
    if step > 0:
        return jnp.concatenate([zero, v[: count - step]], axis=0)
    return jnp.concatenate([v[-step:], zero], axis=0)


def silu_halves(h):
    t = jnp.tanh(h)
    one = 1.0 + t
    return h * one, one * (1.0 + h * (1.0 - t))


def forward_one(recv, spec, pairs, singles, twice, w1, wf, params, masks, all_masks, edge_masks,
                pre_two, payload, act, slopes, x3, stats, features_out, pre_one, got, strips, halo, rows_out):
    devices = recv.shape[0]
    n_mel, count = lax.axis_size("mel"), lax.axis_size("tm")
    rows = MEL_ROWS
    mels = n_mel * rows
    wide = masks.shape[1]
    frame_dev = wide - RIM
    chan = params.shape[1]
    me_m, me_t = lax.axis_index("mel"), lax.axis_index("tm")
    usable, behind, ahead = (masks[n : n + 1] for n in range(3))
    total = masks[3:4, 0:1]
    got[...] = recv[...].astype(F32).reshape(devices * FIRST, 128)

    def every(n):
        return got[pl.ds(n, devices, stride=FIRST), :]

    lane = iota((count, 128), 1)
    bands = [got[pl.ds(FIRST * k * count + COLUMNS, count, stride=FIRST), :] for k in range(n_mel)]
    for c in range(8):
        column = jnp.zeros((count, 128), F32)
        for k, band in enumerate(bands):
            part = jnp.where(lane // rows == c, band, 0.0)
            column = column + (pltpu.roll(part, rows * (k - c) % 128, 1) if k != c else part)
        strips[pl.ds(c, count, stride=8), :] = column
    at = pl.multiple_of(FIRST * (jnp.maximum(me_m - 1, 0) * count + me_t), 8)
    above = got[pl.ds(at, 16), :] * (me_m > 0).astype(F32)
    at = pl.multiple_of(FIRST * (jnp.minimum(me_m + 1, n_mel - 1) * count + me_t), 8)
    below = got[pl.ds(at, 16), :] * (me_m < n_mel - 1).astype(F32)
    above = jnp.concatenate([above[4:8], above[12:16]], axis=1)
    below = jnp.concatenate([below[0:4], below[8:12]], axis=1)
    own = spec[0].astype(F32) * usable[:, :frame_dev]
    at = pl.multiple_of(8 * jnp.minimum(me_t + 1, count - 1), 8)
    after = strips[pl.ds(at, 8), :][:, :mels] * (me_t + 1 < count).astype(F32)
    at = pl.multiple_of(8 * jnp.maximum(me_t - 1, 0), 8)
    before = strips[pl.ds(at, 8), :][:, :mels] * (me_t > 0).astype(F32)
    sides = jnp.concatenate([after[0:4], before[4:8], jnp.zeros((8, mels), F32)], axis=0).astype(BF16)
    side = iota((16, RIM), 0)
    place = iota((16, RIM), 1) == jnp.where(side < 4, side, jnp.where(side < 8, side + RIM - 8, -1))
    halo[0:8] = jnp.zeros((8, RIM), F32)
    halo[mels : mels + 8] = jnp.zeros((8, RIM), F32)
    halo[4 : mels + 4] = dot(sides, place.astype(BF16), ((0,), (0,)))
    rim = halo[pl.ds(pl.multiple_of(me_m * rows, 8), BAND), :]
    near = jnp.concatenate([jnp.concatenate([above, own, below], axis=0), rim], axis=1)
    x3[...] = jnp.concatenate(
        [
            pltpu.roll(near, 1, 1) * behind,
            near,
            pltpu.roll(near, wide - 1, 1) * ahead,
            jnp.broadcast_to(usable, (BAND, wide)),
            jnp.zeros((128 - 4 * BAND, wide), F32),
        ],
        axis=0,
    ).astype(BF16)
    pre_one[...] = dot(w1[...], x3[...])
    lane = iota((1, 128), 1)
    parts = jnp.where(lane < 92, every(SUMS) + every(SUMS + 1) + every(SUMS + 2), 0.0)
    centres, numbers = parts[:, 90:91], parts[:, 91:92]
    centre = jnp.sum(centres * numbers, axis=0, keepdims=True)
    centre = centre / jnp.maximum(jnp.sum(numbers, axis=0, keepdims=True), 1.0)
    delta = centres - centre
    features = jnp.sum(parts + delta * numbers * jnp.where(lane < 81, delta, 1.0), axis=0, keepdims=True)
    moved = jnp.sum(delta * parts, axis=0, keepdims=True)
    def edge_row(k, n):
        first = FIRST * k * count + n
        return jnp.concatenate(
            [got[pl.ds(first, count, stride=FIRST), :], got[pl.ds(first + 8, count, stride=FIRST), :]], axis=1
        )

    edge_rows = [[edge_row(k, n) for n in (0, 1, 6, 7)] for k in range(n_mel)]
    zero = jnp.zeros((count, frame_dev), F32)
    rows_of = [[], [], []]
    for k, (top, second, fore, bottom) in enumerate(edge_rows):
        for n, v in enumerate((edge_rows[k - 1][3] if k else zero, top, second)):
            rows_of[n].append(v)
        for n, v in enumerate((fore, bottom, edge_rows[k + 1][0] if k + 1 < n_mel else zero)):
            rows_of[n].append(v)
    f_usable, f_behind, f_ahead = (all_masks[n * count : (n + 1) * count, :] for n in range(3))
    lane = iota((count, frame_dev), 1)

    def frame_before(v):
        v = pltpu.roll(v, 1, 1)
        return jnp.where(lane == 0, pltpu.roll(v, 1, 0), v) * f_behind

    def frame_after(v):
        v = pltpu.roll(v, frame_dev - 1, 1)
        return jnp.where(lane == frame_dev - 1, pltpu.roll(v, count - 1, 0), v) * f_ahead

    taps = []
    for group in rows_of:
        for move in (frame_before, lambda v: v, frame_after):
            taps.append(jnp.concatenate([move(v) for v in group], axis=1))
    f_usable = jnp.concatenate([f_usable] * (2 * n_mel), axis=1)
    borders = (taps, f_usable)
    edge = strips[...]
    q_usable, q_behind, q_ahead = (edge_masks[:, n : n + 1] for n in range(3))
    lane = iota((count * 8, 128), 1)
    inside = (lane < mels) & (lane % rows != 0) & (lane % rows != rows - 1)
    shifted = [
        pltpu.roll(edge, 1, 0) * q_behind,
        edge,
        pltpu.roll(edge, count * 8 - 1, 0) * q_ahead,
    ]
    taps = [pltpu.roll(v, (1 - i) % 128, 1) if i != 1 else v for i in range(3) for v in shifted]
    features = features + feature_rows(centre, borders, (taps, jnp.where(inside, q_usable, 0.0)))
    features = jnp.where(iota((1, 128), 1) < 90, features, 0.0)
    near_mean = jnp.sum(singles[...] * features, axis=1, keepdims=True) / total
    around = jnp.sum(singles[...], axis=1, keepdims=True)
    square = jnp.sum(pairs[...] * features, axis=1, keepdims=True)
    square = (square + 2.0 * around * jnp.sum(singles[...] * moved, axis=1, keepdims=True)) / total
    inv = lax.rsqrt(square - near_mean * near_mean + 1e-05)
    mean = near_mean + centre * around
    lane = iota((chan, 128), 1)
    stats[0:chan] = jnp.where(lane == 0, mean, jnp.where(lane == 1, inv, 0.0))
    stats[chan : chan + 8] = jnp.broadcast_to(to_lanes(near_mean), (8, 128))
    stats[chan + 8 : chan + 16] = jnp.broadcast_to(to_lanes(inv), (8, 128))
    scale = 0.5 * to_column(params[0:1], chan) * inv
    shift = 0.5 * to_column(params[1:2], chan) - mean * scale
    scale = jnp.broadcast_to(scale, (chan, wide))
    shift = jnp.broadcast_to(shift, (chan, wide))
    ext = w1.shape[0] // chan
    block, taps = wf.shape
    first = jnp.zeros((chan, 128), F32)
    second = jnp.zeros((chan, 128), F32)
    own_mask = usable[:, :frame_dev]
    low_masks = [m.astype(BF16) for m in (usable, behind, ahead)]
    for r in range(ext):
        value, slope = silu_halves(pre_one[r * chan : (r + 1) * chan, :] * scale + shift)
        if 2 <= r < rows + 4:
            mask = 0.5 * usable if 3 <= r < rows + 3 else usable * (0.5 * row_valid(r - 3, rows))
            slopes[(r - 2) * chan : (r - 1) * chan, :] = slope * mask
        if not 0 <= r - 3 < rows:
            value = value * row_valid(r - 3, rows)
        base = r * 3 * chan
        low = value.astype(BF16) * low_masks[0]
        act[base : base + chan, :], act[base + 2 * chan : base + 3 * chan, :] = shifted_frames(low, *low_masks[1:])
        act[base + chan : base + 2 * chan, :] = low
        if r < 3 or r % 2 == 0:
            continue
        g = (r - 3) // 2
        result = dot(wf[...], act[g * 3 * block : g * 3 * block + taps, :])
        pre_two[g * block : (g + 1) * block] = result
        for q in range(2):
            if 2 <= 2 * g + q < rows + 2:
                p = result[q * chan : (q + 1) * chan, :frame_dev]
                masked = p * own_mask
                first = first + halves(masked)
                second = second + halves(masked * p)
    moved = dot(jnp.broadcast_to(moved, (8, 128)), twice[...], precision=EXACT)[0:1]
    features_out[...] = jnp.concatenate(
        [features + moved, jnp.broadcast_to(centre, (1, 128)), jnp.zeros((6, 128), F32)], axis=0
    )
    share = share_of(devices, chan)

    def put(n, value):
        rows_out[pl.ds(n, devices, stride=SECOND), :] = jnp.broadcast_to(value, (devices, 128))

    for n in range(share):
        put(3 + n, moved_rows(every(EDGES + share + n), count))
        put(3 + share + n, moved_rows(every(EDGES + n), -count))
    for n in range(3 + 2 * share, SECOND - 1):
        put(n, jnp.zeros((1, 128), F32))
    lane = iota((devices, 128), 1)
    tm = iota((devices, 128), 0) % count
    lefts = jnp.where(lane >= SIDE, every(SUMS), 0.0)
    rights = jnp.where(lane >= SIDE, every(SUMS + 1), 0.0)
    beside = jnp.zeros((devices, 128), F32)
    for n, step in enumerate((0, count, -count)):
        one = jnp.where(tm > 0, moved_rows(rights, step + 1), 0.0)
        two = jnp.where(tm < count - 1, moved_rows(lefts, step - 1), 0.0)
        beside = beside + pltpu.roll(one, (32 * n - SIDE) % 128, 1) + pltpu.roll(two, (32 * n + 16 - SIDE) % 128, 1)
    put(SECOND - 1, beside)
    first = jnp.sum(first, axis=1, keepdims=True)
    second = jnp.sum(second, axis=1, keepdims=True)
    for n, part in enumerate(three_parts(to_lanes(first) + to_lanes(second, chan))):
        put(n, part)
    payload[...] = rows_out[...].reshape(payload.shape).astype(BF16)


def sum_rows(devices, taps):
    return -(-taps // devices) + 2


def backward_scaled(recv, pre_two, act, own_rows, params, masks,
                    grad, payload, pairs, stats, sides, right, got, beyond):
    devices = recv.shape[0]
    got[...] = recv[...].astype(F32).reshape(devices * SECOND, 128)
    chan = params.shape[1]
    half = own_rows.shape[1]
    lane = iota((half, 2 * half), 1)
    spread = jnp.where(lane >> 1 == iota((half, 2 * half), 0), 0.25, 0.0).astype(BF16)
    rows = MEL_ROWS
    wide = pre_two.shape[1]
    frame_dev = wide - RIM
    usable = masks[0:1]
    share = share_of(devices, chan)
    holders = chan // share

    def every(n):
        return got[pl.ds(n, devices, stride=SECOND), :]

    beside = every(SECOND - 1)[:holders]
    lane = iota((holders, RIM), 1)
    many = rows // 2
    for n in range(share):
        first = n * holders
        beyond[first : first + holders, :] = every(3 + n)[:holders]
        beyond[chan + first : chan + first + holders, :] = every(3 + share + n)[:holders]
        for r in range(many + 2):
            at = many * n + (r if r < many else 32 + many - 1 if r == many else 64)
            left, right_of = beside[:, at : at + 1], beside[:, at + 16 : at + 17]
            side = jnp.where(lane >= RIM - 2, 0.25 * left, jnp.where(lane < 2, 0.25 * right_of, 0.0))
            sides[r * chan + first : r * chan + first + holders, :] = side
    total = masks[3:4, 0:1]
    sums = jnp.sum(every(0) + every(1) + every(2), axis=0, keepdims=True)
    mean = to_column(sums, chan) / total
    inv = lax.rsqrt(to_column(sums, chan, chan) / total - mean * mean + 1e-05)
    lane = iota((chan, 128), 1)
    scale = 0.5 * to_column(params[2:3], chan) * inv
    shift = 0.5 * to_column(params[3:4], chan) - mean * scale
    columns = jnp.zeros((chan, 128), F32)
    for n, column in enumerate((mean, inv, scale, shift)):
        columns = jnp.where(lane == n, column, columns)
    stats[0:chan] = columns
    stats[chan : chan + 8] = jnp.broadcast_to(to_lanes(inv), (8, 128))
    shift = jnp.broadcast_to(shift, (chan, wide))
    scale = jnp.broadcast_to(scale, (chan, wide))
    mean = jnp.broadcast_to(mean, (chan, frame_dev))
    inv = jnp.broadcast_to(inv, (chan, frame_dev))
    first = jnp.zeros((chan, 128), F32)
    second = jnp.zeros((chan, 128), F32)
    own_mask = usable[:, :frame_dev]
    right[3 * chan :] = jnp.ones((16, rows * frame_dev), BF16)
    table = jnp.zeros((9 * chan, 3 * chan + 16), F32)
    for q in list(range(2, rows + 2)) + [0, 1, rows + 2, rows + 3]:
        r = q // 2
        at = slice(q * chan, (q + 1) * chan)
        m = q - 2
        mask = 0.5 * usable if 0 <= m < rows else usable * (0.5 * row_valid(m, rows))
        if q % 2 == 0:
            if 1 <= r <= rows // 2:
                pooled, at_side = own_rows[(r - 1) * chan : r * chan], (r - 1) * chan
            elif r == 0:
                pooled, at_side = beyond[0:chan].astype(BF16), many * chan
            else:
                pooled, at_side = beyond[chan:].astype(BF16), (many + 1) * chan
            up = jnp.concatenate([dot(pooled, spread), sides[at_side : at_side + chan, :]], axis=1)
        pre = pre_two[at, :]
        value, slope = silu_halves(pre * scale + shift)
        g = up * slope * mask
        grad[at, :] = g
        if not 0 <= m < rows:
            continue
        g = g[:, :frame_dev]
        normed = (pre[:, :frame_dev] - mean) * inv
        first = first + halves(g * normed)
        second = second + halves(g)
        value = value[:, :frame_dev] * own_mask
        both = value if m % 2 == 0 else both + value
        if m % 2:
            pairs[(r - 1) * chan : r * chan, :] = both
        lanes = slice(m * frame_dev, (m + 1) * frame_dev)
        right[0:chan, lanes] = g.astype(BF16)
        right[chan : 2 * chan, lanes] = normed.astype(BF16)
        right[2 * chan : 3 * chan, lanes] = (g - right[0:chan, lanes].astype(F32)).astype(BF16)
        if m % 4 == 3:
            left = [act[(n + 2) * 3 * chan : (n + 5) * 3 * chan, :frame_dev] for n in range(m - 3, m + 1)]
            lanes = slice((m - 3) * frame_dev, (m + 1) * frame_dev)
            table = table + dot(jnp.concatenate(left, axis=1), right[:, lanes], ((1,), (1,)))
    first = jnp.sum(first, axis=1, keepdims=True)
    second = jnp.sum(second, axis=1, keepdims=True)
    totals = to_lanes(first) + to_lanes(second, chan)
    block = payload.shape[0] // devices
    payload[pl.ds(0, devices, stride=block), :] = jnp.broadcast_to(totals, (devices, 128))
    rest = jnp.concatenate([table[:, 2 * chan :], jnp.zeros((9 * chan, chan - 16), F32)], axis=1)
    both = table[:, : 2 * chan] + jnp.where(iota(rest.shape, 1) < chan, rest, 0.0)
    single = rest[:, chan : chan + 1]
    lane = iota((devices, 128), 1)
    constants = jnp.zeros((devices, 128), F32)
    for k in range(block - 2):
        cut, ones = both[k * devices : (k + 1) * devices], single[k * devices : (k + 1) * devices]
        short = devices - cut.shape[0]
        if short:
            cut = jnp.concatenate([cut, jnp.zeros((short, 128), F32)], axis=0)
            ones = jnp.concatenate([ones, jnp.zeros((short, 1), F32)], axis=0)
        payload[pl.ds(1 + k, devices, stride=block), :] = cut
        constants = jnp.where(lane == k, ones, constants)
    payload[pl.ds(block - 1, devices, stride=block), :] = constants


def pool(totals, pairs, out, gain_out, bias_out, temp):
    gain_out[...] = totals[0:1, : gain_out.shape[1]]
    bias_out[...] = totals[0:1, gain_out.shape[1] :]
    chan, rows, half = out.shape[1:]
    to_mean = jnp.where(iota((2 * half, half), 0) >> 1 == iota((2 * half, half), 1), 0.25, 0.0)
    pooled = dot(pairs[...], to_mean, precision=EXACT)
    for r in range(rows):
        temp[pl.ds(r, chan, stride=rows), :] = pooled[r * chan : (r + 1) * chan]
    out[0] = temp[...].reshape(chan, rows, half).astype(BF16)


def backward(recv, pre_two, grad, stats_two, slopes, x3, stats, params, masks, wb,
             out, payload, totals, g3, g1):
    chan = params.shape[1]
    rows = MEL_ROWS
    wide = pre_two.shape[1]
    frame_dev = wide - RIM
    usable = masks[0:1]
    behind, ahead = (masks[n : n + 1].astype(BF16) for n in (1, 2))
    total = masks[3:4, 0:1]
    devices = payload.shape[0] // 14

    received = summed_blocks(recv, devices)
    sums = received[0:1]
    gain_sum, bias_sum = sums[:, :chan], sums[:, chan:]
    totals[...] = jnp.broadcast_to(sums, (8, 128))
    mean, inv = stats_two[0:chan, 0:1], stats_two[0:chan, 1:2]
    factor = to_column(params[2:3], chan) * inv
    gain_part = factor * (to_column(sums, chan) / total * inv)
    bias_part = factor * (to_column(sums, chan, chan) / total) - mean * gain_part
    gain_part = jnp.broadcast_to(gain_part, (chan, wide))
    bias_part = jnp.broadcast_to(bias_part, (chan, wide))
    factor = jnp.broadcast_to(factor, (chan, wide))
    factor_one = jnp.broadcast_to(to_column(params[0:1], chan) * stats[0:chan, 1:2], (chan, wide))
    count = pre_two.shape[0] // chan
    table = jnp.zeros((chan, 128), F32)
    for q in range(count):
        at = slice(q * chan, (q + 1) * chan)
        mask = usable if 0 <= q - 2 < rows else usable * row_valid(q - 2, rows)
        low = (factor * grad[at, :] - (bias_part + pre_two[at, :] * gain_part) * mask).astype(BF16)
        base = q * 3 * chan
        g3[base : base + chan, :], g3[base + 2 * chan : base + 3 * chan, :] = shifted_frames(low, behind, ahead)
        g3[base + chan : base + 2 * chan, :] = low
        if q < 3 or q % 2 == 0:
            continue
        start = q - 3
        result = dot(wb[...], g3[start * 3 * chan : (start + 4) * 3 * chan, :])
        for n in range(2):
            m = start + n - 1
            at = slice((m + 1) * chan, (m + 2) * chan)
            value = result[n * chan : (n + 1) * chan] * slopes[at, :]
            out[at, :] = (value * factor_one).astype(BF16)
            if not 0 <= m < rows:
                continue
            g1[m * chan : (m + 1) * chan, :] = value[:, :frame_dev]
            if m % 4 == 3:
                part = g1[(m - 3) * chan : (m + 1) * chan, :]
                high = lax.reduce_precision(part, 8, 7)
                low = (part - high).astype(BF16)
                taps_in = x3[:, :frame_dev]
                products = dot(high.astype(BF16), taps_in, ((1,), (1,))) + dot(low, taps_in, ((1,), (1,)))
                for k in range(4):
                    table = table + pltpu.roll(products[k * chan : (k + 1) * chan], 128 - (m + k), 1)
    tap = iota((16, 128), 0)
    lane = iota((16, 128), 1)
    i = (tap * 11) >> 5
    select = ((lane == BAND * (tap - 3 * i) + i) & (tap < 9)) | ((lane == 3 * BAND) & (tap == 9))
    rows10 = dot(select.astype(F32), table, ((1,), (1,)), EXACT)
    share = received.shape[0] - 2
    mine = received[1 : share + 1]
    single = to_column(received[share + 1 :], share)
    factor_l = params[2:3] * stats_two[chan : chan + 1, :chan]
    mine = mine[:, :chan] - (bias_sum * single + gain_sum * mine[:, chan:]) / total
    mine = factor_l * mine
    lower = -(-share // 2)
    mine = jnp.concatenate([mine] + [jnp.zeros((2 * lower - share, chan), F32)] * (share % 2), axis=0)
    mine = jnp.concatenate([mine[:lower], mine[lower:]], axis=1)
    if lower < 9:
        mine = jnp.concatenate([mine, jnp.zeros((9 - lower, 128), F32)], axis=0)
    sums = jnp.concatenate([rows10[0:5], rows10[5:10]], axis=1)
    block = jnp.concatenate([sums, mine], axis=0)
    block = jnp.concatenate([block] * 4, axis=0)
    for d in range(0, devices, 4):
        payload[14 * d : 14 * (d + 4), :] = block


def transposed(low, w1, x3, stats, masks, ws_hbm, first, normed, ws, pre_one, sem):
    load = pltpu.make_async_copy(ws_hbm, ws, sem)
    load.start()
    chan = low.shape[0] // (MEL_ROWS + 2)
    wide = low.shape[1]
    pre_one[...] = dot(w1[2 * chan : (MEL_ROWS + 4) * chan], x3[...])
    mean = jnp.broadcast_to(stats[0:chan, 0:1], (chan, wide))
    inv = jnp.broadcast_to(stats[0:chan, 1:2], (chan, wide))
    for q in range(MEL_ROWS + 2):
        at = slice(q * chan, (q + 1) * chan)
        mask = masks[0:1] * row_valid(q - 1, MEL_ROWS)
        normed[at, :] = ((pre_one[at, :] - mean) * inv * mask).astype(BF16)
    load.wait()
    first[...] = dot(ws[...], low[...])


def finish(recv, features, stats, k1t, first, normed, ws, params, masks,
           spec_hbm, kernel_one_hbm, kernel_two_hbm, gain_hbm, bias_hbm,
           table, spec_grad, kernel_one, kernel_two, gain_out, bias_out, sems):
    chan = params.shape[1]
    rows = MEL_ROWS
    wide = normed.shape[1]
    frame_dev = wide - RIM
    usable, behind, ahead = (masks[n : n + 1] for n in range(3))
    total = masks[3:4, 0:1]
    gain = params[0:1]
    count = recv.shape[0] // 14
    share = -(-9 * chan // count)
    lower = -(-share // 2)
    left = [recv[pl.ds(5 + p, count, stride=14), :] for p in range(lower)]
    whole = jnp.concatenate([v[:, :chan] for v in left] + [v[:, chan:] for v in left], axis=0)
    for t in range(9):
        kernel_two[t] = whole[t * chan : (t + 1) * chan].T
    stores = [pltpu.make_async_copy(kernel_two, kernel_two_hbm, sems.at[3])]
    stores[0].start()
    sums = summed_blocks(recv, count)[0:5]
    ten = jnp.concatenate([sums[:, :chan], sums[:, chan:]], axis=0)
    bias_sum = ten[9:10]
    mean_l, inv_l = stats[chan : chan + 1, :chan], stats[chan + 8 : chan + 9, :chan]
    ten = ten - features[1:2, 0:1] * bias_sum
    k = k1t[0:9]
    gain_sum = inv_l * (jnp.sum(k * ten[0:9], axis=0, keepdims=True) - mean_l * bias_sum)
    gain_out[...] = gain_sum
    bias_out[...] = bias_sum
    for n, (source, target) in enumerate(((gain_out, gain_hbm), (bias_out, bias_hbm))):
        stores.append(pltpu.make_async_copy(source, target, sems.at[n]))
        stores[-1].start()
    factor_l = gain * inv_l
    scale = factor_l * gain_sum / total
    scale = jnp.concatenate([scale, scale], axis=1)
    scale = jnp.concatenate([scale] * ((rows + 2) // 2), axis=1)
    taps = first[...] - dot((ws[...].astype(F32) * scale).astype(BF16), normed[...])
    for part in range(wide // 128):
        table[part] = taps[:, 128 * part : 128 * (part + 1)]
    moved = [
        jnp.concatenate([table[part, pl.ds(b, rows, stride=8), :] for part in range(wide // 128)], axis=1)
        for b in range(3)
    ]
    constant = jnp.sum(k * (factor_l * bias_sum / total), axis=1, keepdims=True)
    for a in range(3):
        row = iota((rows, 1), 0) + (a - 1) + lax.axis_index("mel") * rows
        valid = ((row >= 0) & (row < lax.axis_size("mel") * rows)).astype(F32) * usable
        for b in range(3):
            t = 3 * (2 - a) + 2 - b
            moved[b] = moved[b] - constant[t : t + 1] * valid
    result = pltpu.roll(moved[0], 1, 1) * behind + moved[1] + pltpu.roll(moved[2], wide - 1, 1) * ahead
    spec_grad[0] = (result * usable)[:, :frame_dev]
    stores.append(pltpu.make_async_copy(spec_grad, spec_hbm, sems.at[2]))
    stores[-1].start()
    row = features[0:1, :]
    lane = iota((1, 128), 1)
    gram = jnp.concatenate(
        [jnp.where(lane < 9, pltpu.roll(row, 128 - 9 * t, 1) if t else row, 0.0) for t in range(9)]
        + [jnp.zeros((7, 128), F32)],
        axis=0,
    )
    single = to_column(row, 16, 81)[0:9]
    k_rows = jnp.concatenate([k1t[...], jnp.zeros((112, chan), F32)], axis=0)
    normed_taps = inv_l * (dot(gram, k_rows, precision=EXACT)[0:9] - single * mean_l)
    grad_taps = factor_l * (ten[0:9] - (bias_sum * single + gain_sum * normed_taps) / total)
    for i in range(3):
        kernel_one[i] = grad_taps[3 * i : 3 * i + 3]
    stores.append(pltpu.make_async_copy(kernel_one, kernel_one_hbm, sems.at[4]))
    stores[-1].start()
    for store in stores:
        store.wait()


def run(kernel, outs, scratch, *args, hbm=0, apart=(), flops=10**8, size=4 * 10**6):
    vmem = pl.BlockSpec(memory_space=pltpu.VMEM)
    devices = lax.axis_size("mel") * lax.axis_size("tm")
    specs = []
    args = list(args)
    for n, a in enumerate(args):
        if hbm and n >= len(args) - hbm:
            specs.append(pl.BlockSpec(memory_space=pltpu.HBM))
            args[n] = pltpu.with_memory_space_constraint(a, pltpu.HBM)
        else:
            specs.append(vmem)
            args[n] = pltpu.with_memory_space_constraint(a, pltpu.VMEM)
    return pl.pallas_call(
        kernel,
        out_shape=outs,
        in_specs=specs,
        out_specs=[pl.BlockSpec(memory_space=pltpu.HBM) if n in apart else vmem for n in range(len(outs))],
        scratch_shapes=scratch,
        compiler_params=pltpu.CompilerParams(vmem_limit_bytes=(29 + devices // 32) * 2**20),
        cost_estimate=pl.CostEstimate(flops=flops, bytes_accessed=size, transcendentals=0),
    )(*args)


def shape(dims, dtype=F32):
    return jax.ShapeDtypeStruct(dims, dtype)


def kept(dims, dtype=F32):
    return pltpu.VMEM(dims, dtype)


def far(dims, dtype=F32):
    return pltpu.HBM(dims, dtype)


def exchange(blocks, axes=AXES):
    return lax.all_to_all(blocks, axes, 0, 0, tiled=True)


def exchange_rows(rows, axes=AXES):
    return exchange(rows[:, None, :], axes)[:, 0, :]


def shards(spectrum, clip_bounds, kernel_one, gain_one, bias_one, kernel_two, gain_two, bias_two, pooled_grad):
    _, rows, frame_dev = spectrum.shape
    chan = kernel_two.shape[0]
    n_mel, n_tm = lax.axis_size("mel"), lax.axis_size("tm")
    devices = n_mel * n_tm
    half = frame_dev // 2
    wide = frame_dev + RIM
    mels = n_mel * rows

    packed, own, spec, masks = run(
        pack,
        [
            kept((devices, FIRST, 128), BF16),
            kept(pooled_grad.shape, BF16),
            kept(spectrum.shape, BF16),
            kept((8, wide)),
        ],
        [
            pltpu.SMEM(clip_bounds.shape, jnp.int32),
            pltpu.VMEM((2 * chan, half), F32),
            pltpu.VMEM((devices * FIRST, 128), F32),
            pltpu.SemaphoreType.DMA((3,)),
        ],
        spectrum,
        pooled_grad,
        clip_bounds,
        hbm=3,
    )
    recv = exchange(packed)
    ext = rows + 6
    span = 4 * 3 * chan
    wf, wb, w1, ws, pairs, singles, k1t, params, all_masks, edge_masks, twice, own_rows = run(
        weights,
        [
            kept((2 * chan, span), BF16),
            kept((2 * chan, span), BF16),
            kept((ext * chan, 128), BF16),
            far((rows * 8, (rows + 2) * chan), BF16),
            kept((chan, 128)),
            kept((chan, 128)),
            kept((16, chan)),
            kept((8, chan)),
            kept((3 * n_tm, frame_dev)),
            kept((n_tm * 8, 128)),
            kept((128, 128)),
            kept((chan * rows // 2, half), BF16),
        ],
        [
            pltpu.VMEM((9, chan, chan), BF16),
            pltpu.VMEM((3, 3, chan), BF16),
            pltpu.VMEM((4, 1, chan), F32),
            pltpu.SMEM(clip_bounds.shape, jnp.int32),
            pltpu.VMEM((rows * 8, (rows + 2) * chan), BF16),
            pltpu.VMEM((chan * rows // 2, half), F32),
            pltpu.SemaphoreType.DMA((8,)),
        ],
        own,
        clip_bounds,
        jnp.transpose(kernel_two, (2, 3, 0, 1)).reshape(9, chan, chan),
        jnp.transpose(kernel_one, (1, 2, 0)),
        gain_one[None],
        bias_one[None],
        gain_two[None],
        bias_two[None],
        hbm=7,
        apart=(3,),
    )
    pre_two, payload, act, slopes, x3, stats_one, features = run(
        forward_one,
        [
            kept(((rows + 4) * chan, wide)),
            kept((devices, SECOND, 128), BF16),
            kept((ext * 3 * chan, wide), BF16),
            kept(((rows + 2) * chan, wide)),
            kept((128, wide), BF16),
            kept((chan + 16, 128)),
            kept((8, 128)),
        ],
        [
            pltpu.VMEM((ext * chan, wide), F32),
            pltpu.VMEM((devices * FIRST, 128), F32),
            pltpu.VMEM((n_tm * 8, 128), F32),
            pltpu.VMEM((mels + 8, RIM), F32),
            pltpu.VMEM((devices * SECOND, 128), F32),
        ],
        recv,
        spec,
        pairs,
        singles,
        twice,
        w1,
        wf,
        params,
        masks,
        all_masks,
        edge_masks,
    )
    recv = exchange(payload)
    grad, payload, row_pairs, stats_two = run(
        backward_scaled,
        [
            kept(((rows + 4) * chan, wide)),
            kept((devices * sum_rows(devices, 9 * chan), 128)),
            kept((rows // 2 * chan, frame_dev)),
            kept((chan + 8, 128)),
        ],
        [
            pltpu.VMEM(((rows // 2 + 2) * chan, RIM), F32),
            pltpu.VMEM((3 * chan + 16, rows * frame_dev), BF16),
            pltpu.VMEM((devices * SECOND, 128), F32),
            pltpu.VMEM((2 * chan, half), F32),
        ],
        recv,
        pre_two,
        act,
        own_rows,
        params,
        masks,
    )
    recv = exchange_rows(payload)
    low, payload, totals = run(
        backward,
        [
            kept(((rows + 2) * chan, wide), BF16),
            kept((devices * 14, 128)),
            kept((8, 128)),
        ],
        [
            pltpu.VMEM(((rows + 4) * 3 * chan, wide), BF16),
            pltpu.VMEM((rows * chan, frame_dev), F32),
        ],
        recv,
        pre_two,
        grad,
        stats_two,
        slopes,
        x3,
        stats_one,
        params,
        masks,
        wb,
    )
    recv = exchange_rows(payload)
    pooled, gain_two_grad, bias_two_grad = run(
        pool,
        [shape((1, chan, rows // 2, half), BF16), shape((1, chan)), shape((1, chan))],
        [
            pltpu.VMEM((rows // 2 * chan, 128), F32),
        ],
        totals,
        row_pairs,
    )
    first, normed, ws = run(
        transposed,
        [
            kept((rows * 8, wide)),
            kept(((rows + 2) * chan, wide), BF16),
            kept((rows * 8, (rows + 2) * chan), BF16),
        ],
        [pltpu.VMEM(((rows + 2) * chan, wide), F32), pltpu.SemaphoreType.DMA],
        low,
        w1,
        x3,
        stats_one,
        masks,
        ws,
        hbm=1,
    )
    spec_grad, kernel_one_grad, kernel_two_grad, gain_one_grad, bias_one_grad = run(
        finish,
        [
            shape((1, rows, frame_dev)),
            shape((3, 3, chan)),
            shape((9, chan, chan)),
            shape((1, chan)),
            shape((1, chan)),
        ],
        [
            pltpu.VMEM((3, rows * 8, 128), F32),
            pltpu.VMEM((1, rows, frame_dev), F32),
            pltpu.VMEM((3, 3, chan), F32),
            pltpu.VMEM((9, chan, chan), F32),
            pltpu.VMEM((1, chan), F32),
            pltpu.VMEM((1, chan), F32),
            pltpu.SemaphoreType.DMA((5,)),
        ],
        recv,
        features,
        stats_one,
        k1t,
        first,
        normed,
        ws,
        params,
        masks,
        apart=range(5),
    )
    kernel_two_grad = jnp.transpose(kernel_two_grad.reshape(3, 3, chan, chan), (2, 3, 0, 1))
    return (
        pooled,
        spec_grad,
        jnp.transpose(kernel_one_grad, (2, 0, 1)),
        gain_one_grad[0],
        bias_one_grad[0],
        kernel_two_grad,
        gain_two_grad[0],
        bias_two_grad[0],
    )


def solution(mesh):
    return jax.shard_map(
        shards,
        mesh=mesh,
        in_specs=(
            P(None, "mel", "tm"),
            P(),
            P(),
            P(),
            P(),
            P(),
            P(),
            P(),
            P(None, None, "mel", "tm"),
        ),
        out_specs=(P(None, None, "mel", "tm"), P(None, "mel", "tm"), P(), P(), P(), P(), P(), P()),
        check_vma=False,
    )
```

```python
import math

import jax
import jax.numpy as jnp
from jax import lax
from jax.experimental import pallas as pl
from jax.experimental.pallas import tpu as pltpu
from jax.sharding import PartitionSpec as P

F32 = jnp.float32
BF16 = jnp.bfloat16
AXES = ("mel", "tm")
EXACT = lax.Precision.HIGHEST
RIM = 128
BAND = 24
MEL_ROWS = 16
FIRST = 24
SUMS, EDGES, COLUMNS = 16, 19, 23
SIDE = 96
SECOND = 8


def iota(shape, dim):
    return lax.broadcasted_iota(jnp.int32, shape, dim)


def dot(a, b, over=((1,), (0,)), precision=None):
    return lax.dot_general(a, b, (over, ((), ())), precision=precision, preferred_element_type=F32)


def to_column(lanes, count, start=0):
    shape = (count, lanes.shape[1])
    return jnp.sum(jnp.where(iota(shape, 1) == iota(shape, 0) + start, lanes, 0.0), axis=1, keepdims=True)


def to_lanes(column, start=0, width=128):
    shape = (column.shape[0], width)
    return jnp.sum(jnp.where(iota(shape, 1) == iota(shape, 0) + start, column, 0.0), axis=0, keepdims=True)


def halves(v):
    total = v[:, :128]
    for n in range(128, v.shape[1], 128):
        total = total + v[:, n : n + 128]
    return total


def frame_masks(bounds, frames):
    last = bounds.shape[1] - 1

    def living(f):
        return (f >= 0) & (f < bounds[0, last])

    def paired(f):
        both = living(f) & living(f + 1)
        for k in range(1, last):
            both = both & (f + 1 != bounds[0, k])
        return both

    return tuple(m.astype(F32) for m in (living(frames), paired(frames - 1), paired(frames)))


def row_valid(row, rows):
    mel = lax.axis_index("mel") * rows + row
    return ((mel >= 0) & (mel < lax.axis_size("mel") * rows)).astype(F32)


def start_all(*pairs, sems):
    copies = [pltpu.make_async_copy(src, dst, sems.at[n]) for n, (src, dst) in enumerate(pairs)]
    for copy in copies:
        copy.start()
    return copies


def wait_all(copies):
    for copy in copies:
        copy.wait()


def shifted_frames(value, behind, ahead):
    wide = value.shape[1]
    return pltpu.roll(value, 1, 1) * behind, pltpu.roll(value, wide - 1, 1) * ahead


def three_parts(v):
    high = lax.reduce_precision(v, 8, 7)
    mid = lax.reduce_precision(v - high, 8, 7)
    return high, mid, v - high - mid


def share_of(devices, chan):
    return -(-chan // devices)


def pack(spec_hbm, grad_hbm, bounds_hbm, out, own, spec, masks, bounds, edges, rows_out, sems):
    copies = start_all((bounds_hbm, bounds), (spec_hbm, spec), (grad_hbm, own), sems=sems)
    copies[0].wait()
    wide = masks.shape[1]
    frame_dev = wide - RIM
    devices = out.shape[0]
    rows = MEL_ROWS
    lane = iota((1, wide), 1)
    frames = lax.axis_index("tm") * frame_dev + jnp.where(lane < frame_dev + RIM // 2, lane, lane - wide)
    last = bounds.shape[1] - 1
    pixels = (bounds[0, last] * (lax.axis_size("mel") * rows)).astype(F32)
    found = frame_masks(bounds, frames)
    masks[...] = jnp.concatenate(
        list(found) + [jnp.full((1, wide), 1.0) * pixels, jnp.zeros((4, wide), F32)], axis=0
    )
    usable, behind, ahead = (m[:, :frame_dev] for m in found)
    copies[1].wait()
    x = spec[0].astype(F32) * usable
    lane = iota((1, frame_dev), 1)
    row = iota((rows, 1), 0)
    inner = jnp.where((lane > 0) & (lane < frame_dev - 1), usable, 0.0)
    number = (rows - 2) * jnp.sum(inner, axis=1, keepdims=True)
    inner = inner * ((row > 0) & (row < rows - 1)).astype(F32)
    centre = jnp.sum(jnp.sum(x, axis=0, keepdims=True), axis=1, keepdims=True)
    centre = centre / (rows * jnp.maximum(jnp.sum(usable, axis=1, keepdims=True), 1.0))
    centre = lax.reduce_precision(centre, 8, 7)
    shifted = [pltpu.roll(x, 1, 1) * behind, x, pltpu.roll(x, frame_dev - 1, 1) * ahead]
    taps = [pltpu.roll(v, (1 - i) % rows, 0) if i != 1 else v for i in range(3) for v in shifted]
    features = feature_rows(centre, (taps, inner))
    lane = iota((1, 128), 1)
    features = jnp.where(lane == 90, centre, jnp.where(lane == 91, number, features))
    pick = iota((8, frame_dev), 0)
    column = jnp.where(pick < 4, pick, frame_dev - 8 + pick)
    strip = dot((iota((8, frame_dev), 1) == column).astype(BF16), x.astype(BF16), ((1,), (1,)))
    lane = iota((8, 128), 1)
    repeat = (iota((rows, 128), 1) % rows == iota((rows, 128), 0)).astype(BF16)
    strip = jnp.where(lane // rows == iota((8, 128), 0), dot(strip.astype(BF16), repeat), 0.0)
    strip = jnp.sum(strip, axis=0, keepdims=True)

    def put(n, value):
        rows_out[pl.ds(n, devices, stride=FIRST), :] = jnp.broadcast_to(value, (devices, 128))

    near = jnp.concatenate([x[0:4], x[rows - 4 :]], axis=0)
    near = jnp.concatenate([near[:, :128], near[:, 128:]], axis=0)
    for d in range(devices):
        rows_out[FIRST * d : FIRST * d + 16, :] = near
    put(COLUMNS, strip)
    copies[2].wait()
    _, chan, many, half = own.shape
    share = share_of(devices, chan)
    holders = chan // share
    g = own[0].astype(F32)
    edges[0:chan] = g[:, 0, :]
    edges[chan:] = g[:, many - 1, :]

    def spread_out(v):
        if holders < devices:
            v = jnp.concatenate([v, jnp.zeros((devices - holders, 128), F32)], axis=0)
        return v

    for n in range(share):
        put(EDGES + n, spread_out(edges[n * holders : (n + 1) * holders, :]))
        put(EDGES + share + n, spread_out(edges[chan + n * holders : chan + (n + 1) * holders, :]))
    for n in range(2 * share, COLUMNS - EDGES):
        put(EDGES + n, jnp.zeros((1, 128), F32))
    end = iota((8, half), 0)
    at = iota((8, half), 1)
    ends = ((end == 0) & (at == 0)) | ((end == 1) & (at == half - 1))
    columns = dot(ends.astype(BF16), g.reshape(chan * many, half).astype(BF16), ((1,), (1,)))
    group = 128 // many
    source = iota((128, 128), 0)
    lane = iota((group, 128), 1)
    mine = lane // many == iota((group, 128), 0)
    parts = three_parts(features)
    for n in range(2):
        side = jnp.zeros((holders, 128), F32)
        for m in range(share):
            move = (iota((128, 128), 1) == SIDE + many * m + source % many).astype(BF16)
            first = m * holders * many // 128
            block = [columns[n : n + 1, 128 * q : 128 * (q + 1)] for q in range(first, first + holders * many // 128)]
            block = jnp.concatenate([jnp.where(mine, v, 0.0) for v in block], axis=0)
            side = side + dot(block.astype(BF16), move)
        put(SUMS + n, spread_out(side) + parts[n])
    put(SUMS + 2, parts[2])
    out[...] = rows_out[...].reshape(out.shape).astype(BF16)


def weights(own, bounds_hbm, k2_hbm, k1_hbm, gain_one_hbm, bias_one_hbm, gain_two_hbm, bias_two_hbm,
            wf, wb, w1, ws_hbm, pairs, singles, k1t, params, all_masks, edge_masks, twice, own_rows,
            k2, k1, vectors, bounds, ws, temp, sems):
    loads = start_all(
        (bounds_hbm, bounds),
        (k2_hbm, k2),
        (k1_hbm, k1),
        (gain_one_hbm, vectors.at[0]),
        (bias_one_hbm, vectors.at[1]),
        (gain_two_hbm, vectors.at[2]),
        (bias_two_hbm, vectors.at[3]),
        sems=sems,
    )
    _, many, count, half = own.shape
    temp[...] = own[0].astype(F32).reshape(many * count, half)
    for r in range(count):
        own_rows[r * many : (r + 1) * many] = temp[pl.ds(r, many, stride=count), :].astype(BF16)
    wait_all(loads)
    chan = k2.shape[1]
    span = wf.shape[1]
    taps = [k2[t].astype(F32) for t in range(9)]
    rest = jnp.zeros((chan, span - 9 * chan), F32)
    forward = jnp.concatenate(taps + [rest], axis=1)
    backward = jnp.concatenate([taps[8 - t].T for t in range(9)] + [rest], axis=1)
    for r in range(wb.shape[0] // chan):
        at = slice(r * chan, (r + 1) * chan)
        wb[at] = (pltpu.roll(backward, 3 * chan * r, 1) if r else backward).astype(BF16)
    full = jnp.concatenate([k1[n].astype(F32) for n in range(3)] + [jnp.zeros((7, chan), F32)], axis=0)
    low = [
        jnp.concatenate([full[3 * (2 - a) + 2 - b : 3 * (2 - a) + 3 - b] for a in range(3)], axis=1)
        for b in range(3)
    ]
    base = jnp.concatenate(low + [jnp.zeros((5, 3 * chan), F32)], axis=0)
    base = jnp.concatenate([base, jnp.zeros((8, ws.shape[1] - 3 * chan), F32)], axis=1)
    for m in range(ws.shape[0] // 8):
        ws[8 * m : 8 * m + 8] = (pltpu.roll(base, chan * m, 1) if m else base).astype(BF16)
    store_ws = pltpu.make_async_copy(ws, ws_hbm, sems.at[7])
    store_ws.start()
    count, frame_dev = all_masks.shape[0] // 3, all_masks.shape[1]
    frames = iota((count, frame_dev), 0) * frame_dev + iota((count, frame_dev), 1)
    for n, mask in enumerate(frame_masks(bounds, frames)):
        all_masks[n * count : (n + 1) * count] = mask
    q = iota(edge_masks.shape, 0)
    lane = iota(edge_masks.shape, 1)
    k = q % 8
    frames = (q // 8) * frame_dev + jnp.where(k < 4, k, k + frame_dev - 8)
    living, behind, ahead = frame_masks(bounds, frames)
    living = jnp.where((k == 0) | (k == 7), living, 0.0)
    edge_masks[...] = jnp.where(lane == 0, living, jnp.where(lane == 1, behind, jnp.where(lane == 2, ahead, 0.0)))
    params[...] = jnp.concatenate(
        [vectors[n] for n in range(4)] + [jnp.zeros((4, chan), F32)], axis=0
    )
    tap = iota((16, 128), 0)
    lane = iota((16, 128), 1)
    i = (tap * 11) >> 5
    ninth = (lane * 57) >> 9
    to_band = (lane == BAND * (tap - 3 * i) + i) & (tap < 9)
    to_left = (ninth == tap) & (tap < 9)
    to_right = (lane - 9 * ninth == tap) & (lane < 81)
    to_single = (lane == 81 + tap) & (tap < 9)
    source = iota((128, 128), 0) - 81
    lane = iota((128, 128), 1)
    ninth = (lane * 57) >> 9
    inside = (source >= 0) & (source < 9) & (lane < 81)
    twice[...] = jnp.where(inside, (source == ninth).astype(F32) + (source == lane - 9 * ninth).astype(F32), 0.0)
    for r in range(wf.shape[0] // chan):
        at = slice(r * chan, (r + 1) * chan)
        wf[at] = (pltpu.roll(forward, 3 * chan * r, 1) if r else forward).astype(BF16)
    k1t[...] = full
    k = full.astype(BF16)
    lanes = [dot(k, select.astype(BF16), ((0,), (0,))) for select in (to_band, to_left, to_right, to_single)]
    pairs[...] = lanes[1] * lanes[2]
    singles[...] = lanes[3]
    for m in range(w1.shape[0] // chan):
        w1[m * chan : (m + 1) * chan] = (pltpu.roll(lanes[0], m, 1) if m else lanes[0]).astype(BF16)
    store_ws.wait()


def feature_rows(centre, *parts):
    def folded(v):
        return jnp.sum(halves(v), axis=0, keepdims=True)

    rows = [jnp.zeros((1, 128), F32)] * 96
    for taps, weight in parts:
        z = [tap - centre for tap in taps]
        for s in range(9):
            left = z[s] * weight
            rows[81 + s] = rows[81 + s] + folded(left)
            for t in range(s, 9):
                rows[9 * s + t] = rows[9 * t + s] = rows[9 * s + t] + folded(left * z[t])
    return to_lanes(jnp.sum(jnp.concatenate(rows, axis=0), axis=1, keepdims=True))


def summed_blocks(ref, devices):
    block = ref.shape[0] // devices
    period = 8 // math.gcd(block, 8)
    step = period * block
    total = ref[0:step, :]
    for at in range(step, ref.shape[0], step):
        total = total + ref[at : at + step, :]
    result = total[0:block]
    for n in range(1, period):
        result = result + total[n * block : (n + 1) * block]
    return result


def moved_rows(v, step):
    if step == 0:
        return v
    count = v.shape[0]
    if abs(step) >= count:
        return jnp.zeros_like(v)
    zero = jnp.zeros((abs(step), v.shape[1]), v.dtype)
    if step > 0:
        return jnp.concatenate([zero, v[: count - step]], axis=0)
    return jnp.concatenate([v[-step:], zero], axis=0)


def silu_halves(h):
    t = jnp.tanh(h)
    one = 1.0 + t
    return h * one, one * (1.0 + h * (1.0 - t))


def forward_one(recv, spec, pairs, singles, twice, w1, wf, params, masks, all_masks, edge_masks,
                pre_two, payload, act, x3, stats, features_out, got, strips, halo, rows_out):
    devices = recv.shape[0]
    n_mel, count = lax.axis_size("mel"), lax.axis_size("tm")
    rows = MEL_ROWS
    mels = n_mel * rows
    wide = masks.shape[1]
    frame_dev = wide - RIM
    chan = params.shape[1]
    me_m, me_t = lax.axis_index("mel"), lax.axis_index("tm")
    usable, behind, ahead = (masks[n : n + 1] for n in range(3))
    total = masks[3:4, 0:1]
    got[...] = recv[...].astype(F32).reshape(devices * FIRST, 128)

    def every(n):
        return got[pl.ds(n, devices, stride=FIRST), :]

    lane = iota((count, 128), 1)
    bands = [got[pl.ds(FIRST * k * count + COLUMNS, count, stride=FIRST), :] for k in range(n_mel)]
    for c in range(8):
        column = jnp.zeros((count, 128), F32)
        for k, band in enumerate(bands):
            part = jnp.where(lane // rows == c, band, 0.0)
            column = column + (pltpu.roll(part, rows * (k - c) % 128, 1) if k != c else part)
        strips[pl.ds(c, count, stride=8), :] = column
    at = pl.multiple_of(FIRST * (jnp.maximum(me_m - 1, 0) * count + me_t), 8)
    above = got[pl.ds(at, 16), :] * (me_m > 0).astype(F32)
    at = pl.multiple_of(FIRST * (jnp.minimum(me_m + 1, n_mel - 1) * count + me_t), 8)
    below = got[pl.ds(at, 16), :] * (me_m < n_mel - 1).astype(F32)
    above = jnp.concatenate([above[4:8], above[12:16]], axis=1)
    below = jnp.concatenate([below[0:4], below[8:12]], axis=1)
    own = spec[0].astype(F32) * usable[:, :frame_dev]
    at = pl.multiple_of(8 * jnp.minimum(me_t + 1, count - 1), 8)
    after = strips[pl.ds(at, 8), :][:, :mels] * (me_t + 1 < count).astype(F32)
    at = pl.multiple_of(8 * jnp.maximum(me_t - 1, 0), 8)
    before = strips[pl.ds(at, 8), :][:, :mels] * (me_t > 0).astype(F32)
    sides = jnp.concatenate([after[0:4], before[4:8], jnp.zeros((8, mels), F32)], axis=0).astype(BF16)
    side = iota((16, RIM), 0)
    place = iota((16, RIM), 1) == jnp.where(side < 4, side, jnp.where(side < 8, side + RIM - 8, -1))
    halo[0:8] = jnp.zeros((8, RIM), F32)
    halo[mels : mels + 8] = jnp.zeros((8, RIM), F32)
    halo[4 : mels + 4] = dot(sides, place.astype(BF16), ((0,), (0,)))
    rim = halo[pl.ds(pl.multiple_of(me_m * rows, 8), BAND), :]
    near = jnp.concatenate([jnp.concatenate([above, own, below], axis=0), rim], axis=1)
    x3[...] = jnp.concatenate(
        [
            pltpu.roll(near, 1, 1) * behind,
            near,
            pltpu.roll(near, wide - 1, 1) * ahead,
            jnp.broadcast_to(usable, (BAND, wide)),
            jnp.zeros((128 - 4 * BAND, wide), F32),
        ],
        axis=0,
    ).astype(BF16)
    lane = iota((1, 128), 1)
    parts = jnp.where(lane < 92, every(SUMS) + every(SUMS + 1) + every(SUMS + 2), 0.0)
    centres, numbers = parts[:, 90:91], parts[:, 91:92]
    centre = jnp.sum(centres * numbers, axis=0, keepdims=True)
    centre = centre / jnp.maximum(jnp.sum(numbers, axis=0, keepdims=True), 1.0)
    delta = centres - centre
    features = jnp.sum(parts + delta * numbers * jnp.where(lane < 81, delta, 1.0), axis=0, keepdims=True)
    moved = jnp.sum(delta * parts, axis=0, keepdims=True)
    def edge_row(k, n):
        first = FIRST * k * count + n
        return jnp.concatenate(
            [got[pl.ds(first, count, stride=FIRST), :], got[pl.ds(first + 8, count, stride=FIRST), :]], axis=1
        )

    edge_rows = [[edge_row(k, n) for n in (0, 1, 6, 7)] for k in range(n_mel)]
    zero = jnp.zeros((count, frame_dev), F32)
    rows_of = [[], [], []]
    for k, (top, second, fore, bottom) in enumerate(edge_rows):
        for n, v in enumerate((edge_rows[k - 1][3] if k else zero, top, second)):
            rows_of[n].append(v)
        for n, v in enumerate((fore, bottom, edge_rows[k + 1][0] if k + 1 < n_mel else zero)):
            rows_of[n].append(v)
    f_usable, f_behind, f_ahead = (all_masks[n * count : (n + 1) * count, :] for n in range(3))
    lane = iota((count, frame_dev), 1)

    def frame_before(v):
        v = pltpu.roll(v, 1, 1)
        return jnp.where(lane == 0, pltpu.roll(v, 1, 0), v) * f_behind

    def frame_after(v):
        v = pltpu.roll(v, frame_dev - 1, 1)
        return jnp.where(lane == frame_dev - 1, pltpu.roll(v, count - 1, 0), v) * f_ahead

    taps = []
    for group in rows_of:
        for move in (frame_before, lambda v: v, frame_after):
            taps.append(jnp.concatenate([move(v) for v in group], axis=1))
    f_usable = jnp.concatenate([f_usable] * (2 * n_mel), axis=1)
    borders = (taps, f_usable)
    edge = strips[...]
    q_usable, q_behind, q_ahead = (edge_masks[:, n : n + 1] for n in range(3))
    lane = iota((count * 8, 128), 1)
    inside = (lane < mels) & (lane % rows != 0) & (lane % rows != rows - 1)
    shifted = [
        pltpu.roll(edge, 1, 0) * q_behind,
        edge,
        pltpu.roll(edge, count * 8 - 1, 0) * q_ahead,
    ]
    taps = [pltpu.roll(v, (1 - i) % 128, 1) if i != 1 else v for i in range(3) for v in shifted]
    features = features + feature_rows(centre, borders, (taps, jnp.where(inside, q_usable, 0.0)))
    features = jnp.where(iota((1, 128), 1) < 90, features, 0.0)
    near_mean = jnp.sum(singles[...] * features, axis=1, keepdims=True) / total
    around = jnp.sum(singles[...], axis=1, keepdims=True)
    square = jnp.sum(pairs[...] * features, axis=1, keepdims=True)
    square = (square + 2.0 * around * jnp.sum(singles[...] * moved, axis=1, keepdims=True)) / total
    inv = lax.rsqrt(square - near_mean * near_mean + 1e-05)
    mean = near_mean + centre * around
    lane = iota((chan, 128), 1)
    stats[0:chan] = jnp.where(lane == 0, mean, jnp.where(lane == 1, inv, 0.0))
    stats[chan : chan + 8] = jnp.broadcast_to(to_lanes(near_mean), (8, 128))
    stats[chan + 8 : chan + 16] = jnp.broadcast_to(to_lanes(inv), (8, 128))
    scale = 0.5 * to_column(params[0:1], chan) * inv
    shift = 0.5 * to_column(params[1:2], chan) - mean * scale
    stats[chan + 16 :] = jnp.where(lane == 0, scale, jnp.where(lane == 1, shift, 0.0))
    scale = jnp.broadcast_to(scale, (chan, wide))
    shift = jnp.broadcast_to(shift, (chan, wide))
    ext = w1.shape[0] // chan
    block, taps = wf.shape
    first = jnp.zeros((chan, 128), F32)
    second = jnp.zeros((chan, 128), F32)
    own_mask = usable[:, :frame_dev]
    low_masks = [m.astype(BF16) for m in (usable, behind, ahead)]
    for r in range(ext):
        if r % 2 == 0:
            pre_one = dot(w1[r * chan : (r + 2) * chan, :], x3[...])
        value, _ = silu_halves(pre_one[r % 2 * chan : (r % 2 + 1) * chan] * scale + shift)
        if not 0 <= r - 3 < rows:
            value = value * row_valid(r - 3, rows)
        base = r * 3 * chan
        low = value.astype(BF16) * low_masks[0]
        act[base : base + chan, :], act[base + 2 * chan : base + 3 * chan, :] = shifted_frames(low, *low_masks[1:])
        act[base + chan : base + 2 * chan, :] = low
        if r < 3 or r % 2 == 0:
            continue
        g = (r - 3) // 2
        result = dot(wf[...], act[g * 3 * block : g * 3 * block + taps, :])
        pre_two[g * block : (g + 1) * block] = result
        for q in range(2):
            if 2 <= 2 * g + q < rows + 2:
                p = result[q * chan : (q + 1) * chan, :frame_dev]
                masked = p * own_mask
                first = first + halves(masked)
                second = second + halves(masked * p)
    moved = dot(jnp.broadcast_to(moved, (8, 128)), twice[...], precision=EXACT)[0:1]
    features_out[...] = jnp.concatenate(
        [features + moved, jnp.broadcast_to(centre, (1, 128)), jnp.zeros((6, 128), F32)], axis=0
    )
    share = share_of(devices, chan)

    def put(n, value):
        rows_out[pl.ds(n, devices, stride=SECOND), :] = jnp.broadcast_to(value, (devices, 128))

    for n in range(share):
        put(3 + n, moved_rows(every(EDGES + share + n), count))
        put(3 + share + n, moved_rows(every(EDGES + n), -count))
    for n in range(3 + 2 * share, SECOND - 1):
        put(n, jnp.zeros((1, 128), F32))
    lane = iota((devices, 128), 1)
    tm = iota((devices, 128), 0) % count
    lefts = jnp.where(lane >= SIDE, every(SUMS), 0.0)
    rights = jnp.where(lane >= SIDE, every(SUMS + 1), 0.0)
    beside = jnp.zeros((devices, 128), F32)
    for n, step in enumerate((0, count, -count)):
        one = jnp.where(tm > 0, moved_rows(rights, step + 1), 0.0)
        two = jnp.where(tm < count - 1, moved_rows(lefts, step - 1), 0.0)
        beside = beside + pltpu.roll(one, (32 * n - SIDE) % 128, 1) + pltpu.roll(two, (32 * n + 16 - SIDE) % 128, 1)
    put(SECOND - 1, beside)
    first = jnp.sum(first, axis=1, keepdims=True)
    second = jnp.sum(second, axis=1, keepdims=True)
    for n, part in enumerate(three_parts(to_lanes(first) + to_lanes(second, chan))):
        put(n, part)
    payload[...] = rows_out[...].reshape(payload.shape).astype(BF16)


def sum_rows(devices, taps):
    return -(-taps // devices) + 2


def backward_scaled(recv, pre_two, act, own_rows, params, masks,
                    grad, payload, pairs, stats, sides, right, got, beyond):
    devices = recv.shape[0]
    got[...] = recv[...].astype(F32).reshape(devices * SECOND, 128)
    chan = params.shape[1]
    half = own_rows.shape[1]
    lane = iota((half, 2 * half), 1)
    spread = jnp.where(lane >> 1 == iota((half, 2 * half), 0), 0.25, 0.0).astype(BF16)
    rows = MEL_ROWS
    wide = pre_two.shape[1]
    frame_dev = wide - RIM
    usable = masks[0:1]
    share = share_of(devices, chan)
    holders = chan // share

    def every(n):
        return got[pl.ds(n, devices, stride=SECOND), :]

    beside = every(SECOND - 1)[:holders]
    lane = iota((holders, RIM), 1)
    many = rows // 2
    for n in range(share):
        first = n * holders
        beyond[first : first + holders, :] = every(3 + n)[:holders]
        beyond[chan + first : chan + first + holders, :] = every(3 + share + n)[:holders]
        for r in range(many + 2):
            at = many * n + (r if r < many else 32 + many - 1 if r == many else 64)
            left, right_of = beside[:, at : at + 1], beside[:, at + 16 : at + 17]
            side = jnp.where(lane >= RIM - 2, 0.25 * left, jnp.where(lane < 2, 0.25 * right_of, 0.0))
            sides[r * chan + first : r * chan + first + holders, :] = side
    total = masks[3:4, 0:1]
    sums = jnp.sum(every(0) + every(1) + every(2), axis=0, keepdims=True)
    mean = to_column(sums, chan) / total
    inv = lax.rsqrt(to_column(sums, chan, chan) / total - mean * mean + 1e-05)
    lane = iota((chan, 128), 1)
    scale = 0.5 * to_column(params[2:3], chan) * inv
    shift = 0.5 * to_column(params[3:4], chan) - mean * scale
    columns = jnp.zeros((chan, 128), F32)
    for n, column in enumerate((mean, inv, scale, shift)):
        columns = jnp.where(lane == n, column, columns)
    stats[0:chan] = columns
    stats[chan : chan + 8] = jnp.broadcast_to(to_lanes(inv), (8, 128))
    shift = jnp.broadcast_to(shift, (chan, wide))
    scale = jnp.broadcast_to(scale, (chan, wide))
    mean = jnp.broadcast_to(mean, (chan, frame_dev))
    inv = jnp.broadcast_to(inv, (chan, frame_dev))
    first = jnp.zeros((chan, 128), F32)
    second = jnp.zeros((chan, 128), F32)
    own_mask = usable[:, :frame_dev]
    right[3 * chan :] = jnp.ones((16, rows * frame_dev), BF16)
    table = jnp.zeros((9 * chan, 3 * chan + 16), F32)
    for q in list(range(2, rows + 2)) + [0, 1, rows + 2, rows + 3]:
        r = q // 2
        at = slice(q * chan, (q + 1) * chan)
        m = q - 2
        mask = 0.5 * usable if 0 <= m < rows else usable * (0.5 * row_valid(m, rows))
        if q % 2 == 0:
            if 1 <= r <= rows // 2:
                pooled, at_side = own_rows[(r - 1) * chan : r * chan], (r - 1) * chan
            elif r == 0:
                pooled, at_side = beyond[0:chan].astype(BF16), many * chan
            else:
                pooled, at_side = beyond[chan:].astype(BF16), (many + 1) * chan
            up = jnp.concatenate([dot(pooled, spread), sides[at_side : at_side + chan, :]], axis=1)
        pre = pre_two[at, :]
        value, slope = silu_halves(pre * scale + shift)
        g = up * slope * mask
        grad[at, :] = g
        if not 0 <= m < rows:
            continue
        g = g[:, :frame_dev]
        normed = (pre[:, :frame_dev] - mean) * inv
        first = first + halves(g * normed)
        second = second + halves(g)
        value = value[:, :frame_dev] * own_mask
        both = value if m % 2 == 0 else both + value
        if m % 2:
            pairs[(r - 1) * chan : r * chan, :] = both
        lanes = slice(m * frame_dev, (m + 1) * frame_dev)
        right[0:chan, lanes] = g.astype(BF16)
        right[chan : 2 * chan, lanes] = normed.astype(BF16)
        right[2 * chan : 3 * chan, lanes] = (g - right[0:chan, lanes].astype(F32)).astype(BF16)
        if m in (5, 11, rows - 1):
            start = m - m % 6
            left = [act[(n + 2) * 3 * chan : (n + 5) * 3 * chan, :frame_dev] for n in range(start, m + 1)]
            lanes = slice(start * frame_dev, (m + 1) * frame_dev)
            table = table + dot(jnp.concatenate(left, axis=1), right[:, lanes], ((1,), (1,)))
    first = jnp.sum(first, axis=1, keepdims=True)
    second = jnp.sum(second, axis=1, keepdims=True)
    totals = to_lanes(first) + to_lanes(second, chan)
    block = payload.shape[0] // devices
    payload[pl.ds(0, devices, stride=block), :] = jnp.broadcast_to(totals, (devices, 128))
    rest = jnp.concatenate([table[:, 2 * chan :], jnp.zeros((9 * chan, chan - 16), F32)], axis=1)
    both = table[:, : 2 * chan] + jnp.where(iota(rest.shape, 1) < chan, rest, 0.0)
    single = rest[:, chan : chan + 1]
    lane = iota((devices, 128), 1)
    constants = jnp.zeros((devices, 128), F32)
    for k in range(block - 2):
        cut, ones = both[k * devices : (k + 1) * devices], single[k * devices : (k + 1) * devices]
        short = devices - cut.shape[0]
        if short:
            cut = jnp.concatenate([cut, jnp.zeros((short, 128), F32)], axis=0)
            ones = jnp.concatenate([ones, jnp.zeros((short, 1), F32)], axis=0)
        payload[pl.ds(1 + k, devices, stride=block), :] = cut
        constants = jnp.where(lane == k, ones, constants)
    payload[pl.ds(block - 1, devices, stride=block), :] = constants


def pool(totals, pairs, out, gain_out, bias_out, temp):
    gain_out[...] = totals[0:1, : gain_out.shape[1]]
    bias_out[...] = totals[0:1, gain_out.shape[1] :]
    chan, rows, half = out.shape[1:]
    to_mean = jnp.where(iota((2 * half, half), 0) >> 1 == iota((2 * half, half), 1), 0.25, 0.0)
    pooled = dot(pairs[...], to_mean, precision=EXACT)
    for r in range(rows):
        temp[pl.ds(r, chan, stride=rows), :] = pooled[r * chan : (r + 1) * chan]
    out[0] = temp[...].reshape(chan, rows, half).astype(BF16)


def backward(recv, pre_two, grad, stats_two, w1, x3, stats, params, masks, wb,
             out, payload, totals, g3, g1):
    chan = params.shape[1]
    rows = MEL_ROWS
    wide = pre_two.shape[1]
    frame_dev = wide - RIM
    usable = masks[0:1]
    behind, ahead = (masks[n : n + 1].astype(BF16) for n in (1, 2))
    total = masks[3:4, 0:1]
    devices = payload.shape[0] // 14

    received = summed_blocks(recv, devices)
    sums = received[0:1]
    gain_sum, bias_sum = sums[:, :chan], sums[:, chan:]
    totals[...] = jnp.broadcast_to(sums, (8, 128))
    mean, inv = stats_two[0:chan, 0:1], stats_two[0:chan, 1:2]
    factor = to_column(params[2:3], chan) * inv
    gain_part = factor * (to_column(sums, chan) / total * inv)
    bias_part = factor * (to_column(sums, chan, chan) / total) - mean * gain_part
    gain_part = jnp.broadcast_to(gain_part, (chan, wide))
    bias_part = jnp.broadcast_to(bias_part, (chan, wide))
    factor = jnp.broadcast_to(factor, (chan, wide))
    scale = jnp.broadcast_to(stats[chan + 16 :, 0:1], (chan, wide))
    shift = jnp.broadcast_to(stats[chan + 16 :, 1:2], (chan, wide))
    factor_one = jnp.broadcast_to(to_column(params[0:1], chan) * stats[0:chan, 1:2], (chan, wide))
    count = pre_two.shape[0] // chan
    table = jnp.zeros((chan, 128), F32)
    for q in range(count):
        at = slice(q * chan, (q + 1) * chan)
        mask = usable if 0 <= q - 2 < rows else usable * row_valid(q - 2, rows)
        low = (factor * grad[at, :] - (bias_part + pre_two[at, :] * gain_part) * mask).astype(BF16)
        base = q * 3 * chan
        g3[base : base + chan, :], g3[base + 2 * chan : base + 3 * chan, :] = shifted_frames(low, behind, ahead)
        g3[base + chan : base + 2 * chan, :] = low
        if q < 3 or q % 2 == 0:
            continue
        start = q - 3
        result = dot(wb[...], g3[start * 3 * chan : (start + 4) * 3 * chan, :])
        pre_one = dot(w1[(start + 2) * chan : (start + 4) * chan, :], x3[...])
        for n in range(2):
            m = start + n - 1
            at = slice((m + 1) * chan, (m + 2) * chan)
            _, slope = silu_halves(pre_one[n * chan : (n + 1) * chan] * scale + shift)
            mask = 0.5 * usable if 0 <= m < rows else usable * (0.5 * row_valid(m, rows))
            value = result[n * chan : (n + 1) * chan] * slope * mask
            out[at, :] = (value * factor_one).astype(BF16)
            if not 0 <= m < rows:
                continue
            g1[m * chan : (m + 1) * chan, :] = value[:, :frame_dev]
            if m % 4 == 3:
                part = g1[(m - 3) * chan : (m + 1) * chan, :]
                high = lax.reduce_precision(part, 8, 7)
                low = (part - high).astype(BF16)
                taps_in = x3[:, :frame_dev]
                products = dot(high.astype(BF16), taps_in, ((1,), (1,))) + dot(low, taps_in, ((1,), (1,)))
                for k in range(4):
                    table = table + pltpu.roll(products[k * chan : (k + 1) * chan], 128 - (m + k), 1)
    tap = iota((16, 128), 0)
    lane = iota((16, 128), 1)
    i = (tap * 11) >> 5
    select = ((lane == BAND * (tap - 3 * i) + i) & (tap < 9)) | ((lane == 3 * BAND) & (tap == 9))
    rows10 = dot(select.astype(F32), table, ((1,), (1,)), EXACT)
    share = received.shape[0] - 2
    mine = received[1 : share + 1]
    single = to_column(received[share + 1 :], share)
    factor_l = params[2:3] * stats_two[chan : chan + 1, :chan]
    mine = mine[:, :chan] - (bias_sum * single + gain_sum * mine[:, chan:]) / total
    mine = factor_l * mine
    lower = -(-share // 2)
    mine = jnp.concatenate([mine] + [jnp.zeros((2 * lower - share, chan), F32)] * (share % 2), axis=0)
    mine = jnp.concatenate([mine[:lower], mine[lower:]], axis=1)
    if lower < 9:
        mine = jnp.concatenate([mine, jnp.zeros((9 - lower, 128), F32)], axis=0)
    sums = jnp.concatenate([rows10[0:5], rows10[5:10]], axis=1)
    block = jnp.concatenate([sums, mine], axis=0)
    block = jnp.concatenate([block] * 4, axis=0)
    for d in range(0, devices, 4):
        payload[14 * d : 14 * (d + 4), :] = block


def transposed(low, w1, x3, stats, masks, ws_hbm, first, normed, ws, sem):
    load = pltpu.make_async_copy(ws_hbm, ws, sem)
    load.start()
    chan = low.shape[0] // (MEL_ROWS + 2)
    wide = low.shape[1]
    mean = jnp.broadcast_to(stats[0:chan, 0:1], (chan, wide))
    inv = jnp.broadcast_to(stats[0:chan, 1:2], (chan, wide))
    for q in range(MEL_ROWS + 2):
        at = slice(q * chan, (q + 1) * chan)
        mask = masks[0:1] * row_valid(q - 1, MEL_ROWS)
        if q % 2 == 0:
            pre_one = dot(w1[(q + 2) * chan : (q + 4) * chan, :], x3[...])
        normed[at, :] = ((pre_one[q % 2 * chan : (q % 2 + 1) * chan] - mean) * inv * mask).astype(BF16)
    load.wait()
    first[...] = dot(ws[...], low[...])


def finish(recv, features, stats, k1t, first, normed, ws, params, masks,
           spec_hbm, kernel_one_hbm, kernel_two_hbm, gain_hbm, bias_hbm,
           table, spec_grad, kernel_one, kernel_two, gain_out, bias_out, sems):
    chan = params.shape[1]
    rows = MEL_ROWS
    wide = normed.shape[1]
    frame_dev = wide - RIM
    usable, behind, ahead = (masks[n : n + 1] for n in range(3))
    total = masks[3:4, 0:1]
    gain = params[0:1]
    count = recv.shape[0] // 14
    share = -(-9 * chan // count)
    lower = -(-share // 2)
    left = [recv[pl.ds(5 + p, count, stride=14), :] for p in range(lower)]
    whole = jnp.concatenate([v[:, :chan] for v in left] + [v[:, chan:] for v in left], axis=0)
    for t in range(9):
        kernel_two[t] = whole[t * chan : (t + 1) * chan].T
    stores = [pltpu.make_async_copy(kernel_two, kernel_two_hbm, sems.at[3])]
    stores[0].start()
    sums = summed_blocks(recv, count)[0:5]
    ten = jnp.concatenate([sums[:, :chan], sums[:, chan:]], axis=0)
    bias_sum = ten[9:10]
    mean_l, inv_l = stats[chan : chan + 1, :chan], stats[chan + 8 : chan + 9, :chan]
    ten = ten - features[1:2, 0:1] * bias_sum
    k = k1t[0:9]
    gain_sum = inv_l * (jnp.sum(k * ten[0:9], axis=0, keepdims=True) - mean_l * bias_sum)
    gain_out[...] = gain_sum
    bias_out[...] = bias_sum
    for n, (source, target) in enumerate(((gain_out, gain_hbm), (bias_out, bias_hbm))):
        stores.append(pltpu.make_async_copy(source, target, sems.at[n]))
        stores[-1].start()
    factor_l = gain * inv_l
    scale = factor_l * gain_sum / total
    scale = jnp.concatenate([scale, scale], axis=1)
    scale = jnp.concatenate([scale] * ((rows + 2) // 2), axis=1)
    taps = first[...] - dot((ws[...].astype(F32) * scale).astype(BF16), normed[...])
    for part in range(wide // 128):
        table[part] = taps[:, 128 * part : 128 * (part + 1)]
    moved = [
        jnp.concatenate([table[part, pl.ds(b, rows, stride=8), :] for part in range(wide // 128)], axis=1)
        for b in range(3)
    ]
    constant = jnp.sum(k * (factor_l * bias_sum / total), axis=1, keepdims=True)
    for a in range(3):
        row = iota((rows, 1), 0) + (a - 1) + lax.axis_index("mel") * rows
        valid = ((row >= 0) & (row < lax.axis_size("mel") * rows)).astype(F32) * usable
        for b in range(3):
            t = 3 * (2 - a) + 2 - b
            moved[b] = moved[b] - constant[t : t + 1] * valid
    result = pltpu.roll(moved[0], 1, 1) * behind + moved[1] + pltpu.roll(moved[2], wide - 1, 1) * ahead
    spec_grad[0] = (result * usable)[:, :frame_dev]
    stores.append(pltpu.make_async_copy(spec_grad, spec_hbm, sems.at[2]))
    stores[-1].start()
    row = features[0:1, :]
    lane = iota((1, 128), 1)
    gram = jnp.concatenate(
        [jnp.where(lane < 9, pltpu.roll(row, 128 - 9 * t, 1) if t else row, 0.0) for t in range(9)]
        + [jnp.zeros((7, 128), F32)],
        axis=0,
    )
    single = to_column(row, 16, 81)[0:9]
    k_rows = jnp.concatenate([k1t[...], jnp.zeros((112, chan), F32)], axis=0)
    normed_taps = inv_l * (dot(gram, k_rows, precision=EXACT)[0:9] - single * mean_l)
    grad_taps = factor_l * (ten[0:9] - (bias_sum * single + gain_sum * normed_taps) / total)
    for i in range(3):
        kernel_one[i] = grad_taps[3 * i : 3 * i + 3]
    stores.append(pltpu.make_async_copy(kernel_one, kernel_one_hbm, sems.at[4]))
    stores[-1].start()
    for store in stores:
        store.wait()


def run(kernel, outs, scratch, *args, hbm=0, apart=(), flops=10**8, size=4 * 10**6):
    vmem = pl.BlockSpec(memory_space=pltpu.VMEM)
    devices = lax.axis_size("mel") * lax.axis_size("tm")
    specs = []
    args = list(args)
    for n, a in enumerate(args):
        if hbm and n >= len(args) - hbm:
            specs.append(pl.BlockSpec(memory_space=pltpu.HBM))
            args[n] = pltpu.with_memory_space_constraint(a, pltpu.HBM)
        else:
            specs.append(vmem)
            args[n] = pltpu.with_memory_space_constraint(a, pltpu.VMEM)
    return pl.pallas_call(
        kernel,
        out_shape=outs,
        in_specs=specs,
        out_specs=[pl.BlockSpec(memory_space=pltpu.HBM) if n in apart else vmem for n in range(len(outs))],
        scratch_shapes=scratch,
        compiler_params=pltpu.CompilerParams(vmem_limit_bytes=(29 + devices // 32) * 2**20),
        cost_estimate=pl.CostEstimate(flops=flops, bytes_accessed=size, transcendentals=0),
    )(*args)


def shape(dims, dtype=F32):
    return jax.ShapeDtypeStruct(dims, dtype)


def kept(dims, dtype=F32):
    return pltpu.VMEM(dims, dtype)


def far(dims, dtype=F32):
    return pltpu.HBM(dims, dtype)


def exchange(blocks, axes=AXES):
    return lax.all_to_all(blocks, axes, 0, 0, tiled=True)


def exchange_rows(rows, axes=AXES):
    return exchange(rows[:, None, :], axes)[:, 0, :]


def shards(spectrum, clip_bounds, kernel_one, gain_one, bias_one, kernel_two, gain_two, bias_two, pooled_grad):
    _, rows, frame_dev = spectrum.shape
    chan = kernel_two.shape[0]
    n_mel, n_tm = lax.axis_size("mel"), lax.axis_size("tm")
    devices = n_mel * n_tm
    half = frame_dev // 2
    wide = frame_dev + RIM
    mels = n_mel * rows

    packed, own, spec, masks = run(
        pack,
        [
            kept((devices, FIRST, 128), BF16),
            kept(pooled_grad.shape, BF16),
            kept(spectrum.shape, BF16),
            kept((8, wide)),
        ],
        [
            pltpu.SMEM(clip_bounds.shape, jnp.int32),
            pltpu.VMEM((2 * chan, half), F32),
            pltpu.VMEM((devices * FIRST, 128), F32),
            pltpu.SemaphoreType.DMA((3,)),
        ],
        spectrum,
        pooled_grad,
        clip_bounds,
        hbm=3,
    )
    recv = exchange(packed)
    ext = rows + 6
    span = 4 * 3 * chan
    wf, wb, w1, ws, pairs, singles, k1t, params, all_masks, edge_masks, twice, own_rows = run(
        weights,
        [
            kept((2 * chan, span), BF16),
            kept((2 * chan, span), BF16),
            kept((ext * chan, 128), BF16),
            far((rows * 8, (rows + 2) * chan), BF16),
            kept((chan, 128)),
            kept((chan, 128)),
            kept((16, chan)),
            kept((8, chan)),
            kept((3 * n_tm, frame_dev)),
            kept((n_tm * 8, 128)),
            kept((128, 128)),
            kept((chan * rows // 2, half), BF16),
        ],
        [
            pltpu.VMEM((9, chan, chan), BF16),
            pltpu.VMEM((3, 3, chan), BF16),
            pltpu.VMEM((4, 1, chan), F32),
            pltpu.SMEM(clip_bounds.shape, jnp.int32),
            pltpu.VMEM((rows * 8, (rows + 2) * chan), BF16),
            pltpu.VMEM((chan * rows // 2, half), F32),
            pltpu.SemaphoreType.DMA((8,)),
        ],
        own,
        clip_bounds,
        jnp.transpose(kernel_two, (2, 3, 0, 1)).reshape(9, chan, chan),
        jnp.transpose(kernel_one, (1, 2, 0)),
        gain_one[None],
        bias_one[None],
        gain_two[None],
        bias_two[None],
        hbm=7,
        apart=(3,),
    )
    pre_two, payload, act, x3, stats_one, features = run(
        forward_one,
        [
            kept(((rows + 4) * chan, wide)),
            kept((devices, SECOND, 128), BF16),
            kept((ext * 3 * chan, wide), BF16),
            kept((128, wide), BF16),
            kept((2 * chan + 16, 128)),
            kept((8, 128)),
        ],
        [
            pltpu.VMEM((devices * FIRST, 128), F32),
            pltpu.VMEM((n_tm * 8, 128), F32),
            pltpu.VMEM((mels + 8, RIM), F32),
            pltpu.VMEM((devices * SECOND, 128), F32),
        ],
        recv,
        spec,
        pairs,
        singles,
        twice,
        w1,
        wf,
        params,
        masks,
        all_masks,
        edge_masks,
    )
    recv = exchange(payload)
    grad, payload, row_pairs, stats_two = run(
        backward_scaled,
        [
            kept(((rows + 4) * chan, wide)),
            kept((devices * sum_rows(devices, 9 * chan), 128)),
            kept((rows // 2 * chan, frame_dev)),
            kept((chan + 8, 128)),
        ],
        [
            pltpu.VMEM(((rows // 2 + 2) * chan, RIM), F32),
            pltpu.VMEM((3 * chan + 16, rows * frame_dev), BF16),
            pltpu.VMEM((devices * SECOND, 128), F32),
            pltpu.VMEM((2 * chan, half), F32),
        ],
        recv,
        pre_two,
        act,
        own_rows,
        params,
        masks,
    )
    recv = exchange_rows(payload)
    low, payload, totals = run(
        backward,
        [
            kept(((rows + 2) * chan, wide), BF16),
            kept((devices * 14, 128)),
            kept((8, 128)),
        ],
        [
            pltpu.VMEM(((rows + 4) * 3 * chan, wide), BF16),
            pltpu.VMEM((rows * chan, frame_dev), F32),
        ],
        recv,
        pre_two,
        grad,
        stats_two,
        w1,
        x3,
        stats_one,
        params,
        masks,
        wb,
    )
    recv = exchange_rows(payload)
    pooled, gain_two_grad, bias_two_grad = run(
        pool,
        [shape((1, chan, rows // 2, half), BF16), shape((1, chan)), shape((1, chan))],
        [
            pltpu.VMEM((rows // 2 * chan, 128), F32),
        ],
        totals,
        row_pairs,
    )
    first, normed, ws = run(
        transposed,
        [
            kept((rows * 8, wide)),
            kept(((rows + 2) * chan, wide), BF16),
            kept((rows * 8, (rows + 2) * chan), BF16),
        ],
        [pltpu.SemaphoreType.DMA],
        low,
        w1,
        x3,
        stats_one,
        masks,
        ws,
        hbm=1,
    )
    spec_grad, kernel_one_grad, kernel_two_grad, gain_one_grad, bias_one_grad = run(
        finish,
        [
            shape((1, rows, frame_dev)),
            shape((3, 3, chan)),
            shape((9, chan, chan)),
            shape((1, chan)),
            shape((1, chan)),
        ],
        [
            pltpu.VMEM((3, rows * 8, 128), F32),
            pltpu.VMEM((1, rows, frame_dev), F32),
            pltpu.VMEM((3, 3, chan), F32),
            pltpu.VMEM((9, chan, chan), F32),
            pltpu.VMEM((1, chan), F32),
            pltpu.VMEM((1, chan), F32),
            pltpu.SemaphoreType.DMA((5,)),
        ],
        recv,
        features,
        stats_one,
        k1t,
        first,
        normed,
        ws,
        params,
        masks,
        apart=range(5),
    )
    kernel_two_grad = jnp.transpose(kernel_two_grad.reshape(3, 3, chan, chan), (2, 3, 0, 1))
    return (
        pooled,
        spec_grad,
        jnp.transpose(kernel_one_grad, (2, 0, 1)),
        gain_one_grad[0],
        bias_one_grad[0],
        kernel_two_grad,
        gain_two_grad[0],
        bias_two_grad[0],
    )


def solution(mesh):
    return jax.shard_map(
        shards,
        mesh=mesh,
        in_specs=(
            P(None, "mel", "tm"),
            P(),
            P(),
            P(),
            P(),
            P(),
            P(),
            P(),
            P(None, None, "mel", "tm"),
        ),
        out_specs=(P(None, None, "mel", "tm"), P(None, "mel", "tm"), P(), P(), P(), P(), P(), P()),
        check_vma=False,
    )
```

```python
import math

import jax
import jax.numpy as jnp
from jax import lax
from jax.experimental import pallas as pl
from jax.experimental.pallas import tpu as pltpu
from jax.sharding import PartitionSpec as P

F32 = jnp.float32
BF16 = jnp.bfloat16
AXES = ("mel", "tm")
EXACT = lax.Precision.HIGHEST
RIM = 128
BAND = 24
MEL_ROWS = 16
FIRST = 24
SUMS, EDGES, COLUMNS = 16, 19, 23
SIDE = 96
SECOND = 8


def iota(shape, dim):
    return lax.broadcasted_iota(jnp.int32, shape, dim)


def dot(a, b, over=((1,), (0,)), precision=None):
    return lax.dot_general(a, b, (over, ((), ())), precision=precision, preferred_element_type=F32)


def to_column(lanes, count, start=0):
    shape = (count, lanes.shape[1])
    return jnp.sum(jnp.where(iota(shape, 1) == iota(shape, 0) + start, lanes, 0.0), axis=1, keepdims=True)


def to_lanes(column, start=0, width=128):
    shape = (column.shape[0], width)
    return jnp.sum(jnp.where(iota(shape, 1) == iota(shape, 0) + start, column, 0.0), axis=0, keepdims=True)


def halves(v):
    total = v[:, :128]
    for n in range(128, v.shape[1], 128):
        total = total + v[:, n : n + 128]
    return total


def frame_masks(bounds, frames):
    last = bounds.shape[1] - 1

    def living(f):
        return (f >= 0) & (f < bounds[0, last])

    def paired(f):
        both = living(f) & living(f + 1)
        for k in range(1, last):
            both = both & (f + 1 != bounds[0, k])
        return both

    return tuple(m.astype(F32) for m in (living(frames), paired(frames - 1), paired(frames)))


def row_valid(row, rows):
    mel = lax.axis_index("mel") * rows + row
    return ((mel >= 0) & (mel < lax.axis_size("mel") * rows)).astype(F32)


def start_all(*pairs, sems):
    copies = [pltpu.make_async_copy(src, dst, sems.at[n]) for n, (src, dst) in enumerate(pairs)]
    for copy in copies:
        copy.start()
    return copies


def wait_all(copies):
    for copy in copies:
        copy.wait()


def shifted_frames(value, behind, ahead):
    wide = value.shape[1]
    return pltpu.roll(value, 1, 1) * behind, pltpu.roll(value, wide - 1, 1) * ahead


def three_parts(v):
    high = lax.reduce_precision(v, 8, 7)
    mid = lax.reduce_precision(v - high, 8, 7)
    return high, mid, v - high - mid


def share_of(devices, chan):
    return -(-chan // devices)


def pack(spec_hbm, grad_hbm, bounds_hbm, out, own, spec, masks, bounds, edges, rows_out, sems):
    copies = start_all((bounds_hbm, bounds), (spec_hbm, spec), (grad_hbm, own), sems=sems)
    copies[0].wait()
    wide = masks.shape[1]
    frame_dev = wide - RIM
    devices = out.shape[0]
    rows = MEL_ROWS
    lane = iota((1, wide), 1)
    frames = lax.axis_index("tm") * frame_dev + jnp.where(lane < frame_dev + RIM // 2, lane, lane - wide)
    last = bounds.shape[1] - 1
    pixels = (bounds[0, last] * (lax.axis_size("mel") * rows)).astype(F32)
    found = frame_masks(bounds, frames)
    masks[...] = jnp.concatenate(
        list(found) + [jnp.full((1, wide), 1.0) * pixels, jnp.zeros((4, wide), F32)], axis=0
    )
    usable, behind, ahead = (m[:, :frame_dev] for m in found)
    copies[1].wait()
    x = spec[0].astype(F32) * usable
    lane = iota((1, frame_dev), 1)
    row = iota((rows, 1), 0)
    inner = jnp.where((lane > 0) & (lane < frame_dev - 1), usable, 0.0)
    number = (rows - 2) * jnp.sum(inner, axis=1, keepdims=True)
    inner = inner * ((row > 0) & (row < rows - 1)).astype(F32)
    centre = jnp.sum(jnp.sum(x, axis=0, keepdims=True), axis=1, keepdims=True)
    centre = centre / (rows * jnp.maximum(jnp.sum(usable, axis=1, keepdims=True), 1.0))
    centre = lax.reduce_precision(centre, 8, 7)
    shifted = [pltpu.roll(x, 1, 1) * behind, x, pltpu.roll(x, frame_dev - 1, 1) * ahead]
    taps = [pltpu.roll(v, (1 - i) % rows, 0) if i != 1 else v for i in range(3) for v in shifted]
    features = feature_rows(centre, (taps, inner))
    lane = iota((1, 128), 1)
    features = jnp.where(lane == 90, centre, jnp.where(lane == 91, number, features))
    pick = iota((8, frame_dev), 0)
    column = jnp.where(pick < 4, pick, frame_dev - 8 + pick)
    strip = dot((iota((8, frame_dev), 1) == column).astype(BF16), x.astype(BF16), ((1,), (1,)))
    lane = iota((8, 128), 1)
    repeat = (iota((rows, 128), 1) % rows == iota((rows, 128), 0)).astype(BF16)
    strip = jnp.where(lane // rows == iota((8, 128), 0), dot(strip.astype(BF16), repeat), 0.0)
    strip = jnp.sum(strip, axis=0, keepdims=True)

    def put(n, value):
        rows_out[pl.ds(n, devices, stride=FIRST), :] = jnp.broadcast_to(value, (devices, 128))

    near = jnp.concatenate([x[0:4], x[rows - 4 :]], axis=0)
    near = jnp.concatenate([near[:, :128], near[:, 128:]], axis=0)
    for d in range(devices):
        rows_out[FIRST * d : FIRST * d + 16, :] = near
    put(COLUMNS, strip)
    copies[2].wait()
    _, chan, many, half = own.shape
    share = share_of(devices, chan)
    holders = chan // share
    g = own[0].astype(F32)
    edges[0:chan] = g[:, 0, :]
    edges[chan:] = g[:, many - 1, :]

    def spread_out(v):
        if holders < devices:
            v = jnp.concatenate([v, jnp.zeros((devices - holders, 128), F32)], axis=0)
        return v

    for n in range(share):
        put(EDGES + n, spread_out(edges[n * holders : (n + 1) * holders, :]))
        put(EDGES + share + n, spread_out(edges[chan + n * holders : chan + (n + 1) * holders, :]))
    for n in range(2 * share, COLUMNS - EDGES):
        put(EDGES + n, jnp.zeros((1, 128), F32))
    end = iota((8, half), 0)
    at = iota((8, half), 1)
    ends = ((end == 0) & (at == 0)) | ((end == 1) & (at == half - 1))
    columns = dot(ends.astype(BF16), g.reshape(chan * many, half).astype(BF16), ((1,), (1,)))
    group = 128 // many
    source = iota((128, 128), 0)
    lane = iota((group, 128), 1)
    mine = lane // many == iota((group, 128), 0)
    parts = three_parts(features)
    for n in range(2):
        side = jnp.zeros((holders, 128), F32)
        for m in range(share):
            move = (iota((128, 128), 1) == SIDE + many * m + source % many).astype(BF16)
            first = m * holders * many // 128
            block = [columns[n : n + 1, 128 * q : 128 * (q + 1)] for q in range(first, first + holders * many // 128)]
            block = jnp.concatenate([jnp.where(mine, v, 0.0) for v in block], axis=0)
            side = side + dot(block.astype(BF16), move)
        put(SUMS + n, spread_out(side) + parts[n])
    put(SUMS + 2, parts[2])
    out[...] = rows_out[...].reshape(out.shape).astype(BF16)


def weights(own, bounds_hbm, k2_hbm, k1_hbm, gain_one_hbm, bias_one_hbm, gain_two_hbm, bias_two_hbm,
            wf, wb, w1, ws_hbm, pairs, singles, k1t, params, all_masks, edge_masks, twice, own_rows,
            k2, k1, vectors, bounds, ws, temp, sems):
    loads = start_all(
        (bounds_hbm, bounds),
        (k2_hbm, k2),
        (k1_hbm, k1),
        (gain_one_hbm, vectors.at[0]),
        (bias_one_hbm, vectors.at[1]),
        (gain_two_hbm, vectors.at[2]),
        (bias_two_hbm, vectors.at[3]),
        sems=sems,
    )
    _, many, count, half = own.shape
    temp[...] = own[0].astype(F32).reshape(many * count, half)
    for r in range(count):
        own_rows[r * many : (r + 1) * many] = temp[pl.ds(r, many, stride=count), :].astype(BF16)
    wait_all(loads)
    chan = k2.shape[1]
    span = wf.shape[1]
    taps = [k2[t].astype(F32) for t in range(9)]
    rest = jnp.zeros((chan, span - 9 * chan), F32)
    forward = jnp.concatenate(taps + [rest], axis=1)
    backward = jnp.concatenate([taps[8 - t].T for t in range(9)] + [rest], axis=1)
    for r in range(wb.shape[0] // chan):
        at = slice(r * chan, (r + 1) * chan)
        wb[at] = (pltpu.roll(backward, 3 * chan * r, 1) if r else backward).astype(BF16)
    full = jnp.concatenate([k1[n].astype(F32) for n in range(3)] + [jnp.zeros((7, chan), F32)], axis=0)
    low = [
        jnp.concatenate([full[3 * (2 - a) + 2 - b : 3 * (2 - a) + 3 - b] for a in range(3)], axis=1)
        for b in range(3)
    ]
    base = jnp.concatenate(low + [jnp.zeros((5, 3 * chan), F32)], axis=0)
    base = jnp.concatenate([base, jnp.zeros((8, ws.shape[1] - 3 * chan), F32)], axis=1)
    for m in range(ws.shape[0] // 8):
        ws[8 * m : 8 * m + 8] = (pltpu.roll(base, chan * m, 1) if m else base).astype(BF16)
    store_ws = pltpu.make_async_copy(ws, ws_hbm, sems.at[7])
    store_ws.start()
    count, frame_dev = all_masks.shape[0] // 3, all_masks.shape[1]
    frames = iota((count, frame_dev), 0) * frame_dev + iota((count, frame_dev), 1)
    for n, mask in enumerate(frame_masks(bounds, frames)):
        all_masks[n * count : (n + 1) * count] = mask
    q = iota(edge_masks.shape, 0)
    lane = iota(edge_masks.shape, 1)
    k = q % 8
    frames = (q // 8) * frame_dev + jnp.where(k < 4, k, k + frame_dev - 8)
    living, behind, ahead = frame_masks(bounds, frames)
    living = jnp.where((k == 0) | (k == 7), living, 0.0)
    edge_masks[...] = jnp.where(lane == 0, living, jnp.where(lane == 1, behind, jnp.where(lane == 2, ahead, 0.0)))
    params[...] = jnp.concatenate(
        [vectors[n] for n in range(4)] + [jnp.zeros((4, chan), F32)], axis=0
    )
    tap = iota((16, 128), 0)
    lane = iota((16, 128), 1)
    i = (tap * 11) >> 5
    ninth = (lane * 57) >> 9
    to_band = (lane == BAND * (tap - 3 * i) + i) & (tap < 9)
    to_left = (ninth == tap) & (tap < 9)
    to_right = (lane - 9 * ninth == tap) & (lane < 81)
    to_single = (lane == 81 + tap) & (tap < 9)
    source = iota((128, 128), 0) - 81
    lane = iota((128, 128), 1)
    ninth = (lane * 57) >> 9
    inside = (source >= 0) & (source < 9) & (lane < 81)
    twice[...] = jnp.where(inside, (source == ninth).astype(F32) + (source == lane - 9 * ninth).astype(F32), 0.0)
    for r in range(wf.shape[0] // chan):
        at = slice(r * chan, (r + 1) * chan)
        wf[at] = (pltpu.roll(forward, 3 * chan * r, 1) if r else forward).astype(BF16)
    k1t[...] = full
    k = full.astype(BF16)
    lanes = [dot(k, select.astype(BF16), ((0,), (0,))) for select in (to_band, to_left, to_right, to_single)]
    pairs[...] = lanes[1] * lanes[2]
    singles[...] = lanes[3]
    for m in range(w1.shape[0] // chan):
        w1[m * chan : (m + 1) * chan] = (pltpu.roll(lanes[0], m, 1) if m else lanes[0]).astype(BF16)
    store_ws.wait()


def feature_rows(centre, *parts):
    def folded(v):
        return jnp.sum(halves(v), axis=0, keepdims=True)

    rows = [jnp.zeros((1, 128), F32)] * 96
    for taps, weight in parts:
        z = [tap - centre for tap in taps]
        for s in range(9):
            left = z[s] * weight
            rows[81 + s] = rows[81 + s] + folded(left)
            for t in range(s, 9):
                rows[9 * s + t] = rows[9 * t + s] = rows[9 * s + t] + folded(left * z[t])
    return to_lanes(jnp.sum(jnp.concatenate(rows, axis=0), axis=1, keepdims=True))


def summed_blocks(ref, devices):
    block = ref.shape[0] // devices
    period = 8 // math.gcd(block, 8)
    step = period * block
    total = ref[0:step, :]
    for at in range(step, ref.shape[0], step):
        total = total + ref[at : at + step, :]
    result = total[0:block]
    for n in range(1, period):
        result = result + total[n * block : (n + 1) * block]
    return result


def moved_rows(v, step):
    if step == 0:
        return v
    count = v.shape[0]
    if abs(step) >= count:
        return jnp.zeros_like(v)
    zero = jnp.zeros((abs(step), v.shape[1]), v.dtype)
    if step > 0:
        return jnp.concatenate([zero, v[: count - step]], axis=0)
    return jnp.concatenate([v[-step:], zero], axis=0)


def silu_halves(h):
    t = jnp.tanh(h)
    one = 1.0 + t
    return h * one, one * (1.0 + h * (1.0 - t))


def forward_one(recv, spec, pairs, singles, twice, w1, wf, params, masks, all_masks, edge_masks,
                pre_two, payload, act, x3, stats, features_out, pre_one, got, strips, halo, rows_out):
    devices = recv.shape[0]
    n_mel, count = lax.axis_size("mel"), lax.axis_size("tm")
    rows = MEL_ROWS
    mels = n_mel * rows
    wide = masks.shape[1]
    frame_dev = wide - RIM
    chan = params.shape[1]
    me_m, me_t = lax.axis_index("mel"), lax.axis_index("tm")
    usable, behind, ahead = (masks[n : n + 1] for n in range(3))
    total = masks[3:4, 0:1]
    got[...] = recv[...].astype(F32).reshape(devices * FIRST, 128)

    def every(n):
        return got[pl.ds(n, devices, stride=FIRST), :]

    lane = iota((count, 128), 1)
    bands = [got[pl.ds(FIRST * k * count + COLUMNS, count, stride=FIRST), :] for k in range(n_mel)]
    for c in range(8):
        column = jnp.zeros((count, 128), F32)
        for k, band in enumerate(bands):
            part = jnp.where(lane // rows == c, band, 0.0)
            column = column + (pltpu.roll(part, rows * (k - c) % 128, 1) if k != c else part)
        strips[pl.ds(c, count, stride=8), :] = column
    at = pl.multiple_of(FIRST * (jnp.maximum(me_m - 1, 0) * count + me_t), 8)
    above = got[pl.ds(at, 16), :] * (me_m > 0).astype(F32)
    at = pl.multiple_of(FIRST * (jnp.minimum(me_m + 1, n_mel - 1) * count + me_t), 8)
    below = got[pl.ds(at, 16), :] * (me_m < n_mel - 1).astype(F32)
    above = jnp.concatenate([above[4:8], above[12:16]], axis=1)
    below = jnp.concatenate([below[0:4], below[8:12]], axis=1)
    own = spec[0].astype(F32) * usable[:, :frame_dev]
    at = pl.multiple_of(8 * jnp.minimum(me_t + 1, count - 1), 8)
    after = strips[pl.ds(at, 8), :][:, :mels] * (me_t + 1 < count).astype(F32)
    at = pl.multiple_of(8 * jnp.maximum(me_t - 1, 0), 8)
    before = strips[pl.ds(at, 8), :][:, :mels] * (me_t > 0).astype(F32)
    sides = jnp.concatenate([after[0:4], before[4:8], jnp.zeros((8, mels), F32)], axis=0).astype(BF16)
    side = iota((16, RIM), 0)
    place = iota((16, RIM), 1) == jnp.where(side < 4, side, jnp.where(side < 8, side + RIM - 8, -1))
    halo[0:8] = jnp.zeros((8, RIM), F32)
    halo[mels : mels + 8] = jnp.zeros((8, RIM), F32)
    halo[4 : mels + 4] = dot(sides, place.astype(BF16), ((0,), (0,)))
    rim = halo[pl.ds(pl.multiple_of(me_m * rows, 8), BAND), :]
    near = jnp.concatenate([jnp.concatenate([above, own, below], axis=0), rim], axis=1)
    x3[...] = jnp.concatenate(
        [
            pltpu.roll(near, 1, 1) * behind,
            near,
            pltpu.roll(near, wide - 1, 1) * ahead,
            jnp.broadcast_to(usable, (BAND, wide)),
            jnp.zeros((128 - 4 * BAND, wide), F32),
        ],
        axis=0,
    ).astype(BF16)
    pre_one[...] = dot(w1[...], x3[...])
    lane = iota((1, 128), 1)
    parts = jnp.where(lane < 92, every(SUMS) + every(SUMS + 1) + every(SUMS + 2), 0.0)
    centres, numbers = parts[:, 90:91], parts[:, 91:92]
    centre = jnp.sum(centres * numbers, axis=0, keepdims=True)
    centre = centre / jnp.maximum(jnp.sum(numbers, axis=0, keepdims=True), 1.0)
    delta = centres - centre
    features = jnp.sum(parts + delta * numbers * jnp.where(lane < 81, delta, 1.0), axis=0, keepdims=True)
    moved = jnp.sum(delta * parts, axis=0, keepdims=True)
    def edge_row(k, n):
        first = FIRST * k * count + n
        return jnp.concatenate(
            [got[pl.ds(first, count, stride=FIRST), :], got[pl.ds(first + 8, count, stride=FIRST), :]], axis=1
        )

    edge_rows = [[edge_row(k, n) for n in (0, 1, 6, 7)] for k in range(n_mel)]
    zero = jnp.zeros((count, frame_dev), F32)
    rows_of = [[], [], []]
    for k, (top, second, fore, bottom) in enumerate(edge_rows):
        for n, v in enumerate((edge_rows[k - 1][3] if k else zero, top, second)):
            rows_of[n].append(v)
        for n, v in enumerate((fore, bottom, edge_rows[k + 1][0] if k + 1 < n_mel else zero)):
            rows_of[n].append(v)
    f_usable, f_behind, f_ahead = (all_masks[n * count : (n + 1) * count, :] for n in range(3))
    lane = iota((count, frame_dev), 1)

    def frame_before(v):
        v = pltpu.roll(v, 1, 1)
        return jnp.where(lane == 0, pltpu.roll(v, 1, 0), v) * f_behind

    def frame_after(v):
        v = pltpu.roll(v, frame_dev - 1, 1)
        return jnp.where(lane == frame_dev - 1, pltpu.roll(v, count - 1, 0), v) * f_ahead

    taps = []
    for group in rows_of:
        for move in (frame_before, lambda v: v, frame_after):
            taps.append(jnp.concatenate([move(v) for v in group], axis=1))
    f_usable = jnp.concatenate([f_usable] * (2 * n_mel), axis=1)
    borders = (taps, f_usable)
    edge = strips[...]
    q_usable, q_behind, q_ahead = (edge_masks[:, n : n + 1] for n in range(3))
    lane = iota((count * 8, 128), 1)
    inside = (lane < mels) & (lane % rows != 0) & (lane % rows != rows - 1)
    shifted = [
        pltpu.roll(edge, 1, 0) * q_behind,
        edge,
        pltpu.roll(edge, count * 8 - 1, 0) * q_ahead,
    ]
    taps = [pltpu.roll(v, (1 - i) % 128, 1) if i != 1 else v for i in range(3) for v in shifted]
    features = features + feature_rows(centre, borders, (taps, jnp.where(inside, q_usable, 0.0)))
    features = jnp.where(iota((1, 128), 1) < 90, features, 0.0)
    near_mean = jnp.sum(singles[...] * features, axis=1, keepdims=True) / total
    around = jnp.sum(singles[...], axis=1, keepdims=True)
    square = jnp.sum(pairs[...] * features, axis=1, keepdims=True)
    square = (square + 2.0 * around * jnp.sum(singles[...] * moved, axis=1, keepdims=True)) / total
    inv = lax.rsqrt(square - near_mean * near_mean + 1e-05)
    mean = near_mean + centre * around
    lane = iota((chan, 128), 1)
    stats[0:chan] = jnp.where(lane == 0, mean, jnp.where(lane == 1, inv, 0.0))
    stats[chan : chan + 8] = jnp.broadcast_to(to_lanes(near_mean), (8, 128))
    stats[chan + 8 : chan + 16] = jnp.broadcast_to(to_lanes(inv), (8, 128))
    scale = 0.5 * to_column(params[0:1], chan) * inv
    shift = 0.5 * to_column(params[1:2], chan) - mean * scale
    stats[chan + 16 :] = jnp.where(lane == 0, scale, jnp.where(lane == 1, shift, 0.0))
    scale = jnp.broadcast_to(scale, (chan, wide))
    shift = jnp.broadcast_to(shift, (chan, wide))
    ext = w1.shape[0] // chan
    block, taps = wf.shape
    first = jnp.zeros((chan, 128), F32)
    second = jnp.zeros((chan, 128), F32)
    own_mask = usable[:, :frame_dev]
    low_masks = [m.astype(BF16) for m in (usable, behind, ahead)]
    for r in range(ext):
        value, _ = silu_halves(pre_one[r * chan : (r + 1) * chan, :] * scale + shift)
        if not 0 <= r - 3 < rows:
            value = value * row_valid(r - 3, rows)
        base = r * 3 * chan
        low = value.astype(BF16) * low_masks[0]
        act[base : base + chan, :], act[base + 2 * chan : base + 3 * chan, :] = shifted_frames(low, *low_masks[1:])
        act[base + chan : base + 2 * chan, :] = low
        if r < 3 or r % 2 == 0:
            continue
        g = (r - 3) // 2
        result = dot(wf[...], act[g * 3 * block : g * 3 * block + taps, :])
        pre_two[g * block : (g + 1) * block] = result
        for q in range(2):
            if 2 <= 2 * g + q < rows + 2:
                p = result[q * chan : (q + 1) * chan, :frame_dev]
                masked = p * own_mask
                first = first + halves(masked)
                second = second + halves(masked * p)
    moved = dot(jnp.broadcast_to(moved, (8, 128)), twice[...], precision=EXACT)[0:1]
    features_out[...] = jnp.concatenate(
        [features + moved, jnp.broadcast_to(centre, (1, 128)), jnp.zeros((6, 128), F32)], axis=0
    )
    share = share_of(devices, chan)

    def put(n, value):
        rows_out[pl.ds(n, devices, stride=SECOND), :] = jnp.broadcast_to(value, (devices, 128))

    for n in range(share):
        put(3 + n, moved_rows(every(EDGES + share + n), count))
        put(3 + share + n, moved_rows(every(EDGES + n), -count))
    for n in range(3 + 2 * share, SECOND - 1):
        put(n, jnp.zeros((1, 128), F32))
    lane = iota((devices, 128), 1)
    tm = iota((devices, 128), 0) % count
    lefts = jnp.where(lane >= SIDE, every(SUMS), 0.0)
    rights = jnp.where(lane >= SIDE, every(SUMS + 1), 0.0)
    beside = jnp.zeros((devices, 128), F32)
    for n, step in enumerate((0, count, -count)):
        one = jnp.where(tm > 0, moved_rows(rights, step + 1), 0.0)
        two = jnp.where(tm < count - 1, moved_rows(lefts, step - 1), 0.0)
        beside = beside + pltpu.roll(one, (32 * n - SIDE) % 128, 1) + pltpu.roll(two, (32 * n + 16 - SIDE) % 128, 1)
    put(SECOND - 1, beside)
    first = jnp.sum(first, axis=1, keepdims=True)
    second = jnp.sum(second, axis=1, keepdims=True)
    for n, part in enumerate(three_parts(to_lanes(first) + to_lanes(second, chan))):
        put(n, part)
    payload[...] = rows_out[...].reshape(payload.shape).astype(BF16)


def sum_rows(devices, taps):
    return -(-taps // devices) + 2


def backward_scaled(recv, pre_two, act, own_rows, params, masks,
                    grad, payload, pairs, stats, sides, up, right, got, beyond):
    devices = recv.shape[0]
    got[...] = recv[...].astype(F32).reshape(devices * SECOND, 128)
    chan = params.shape[1]
    half = own_rows.shape[1]
    lane = iota((half, 2 * half), 1)
    spread = jnp.where(lane >> 1 == iota((half, 2 * half), 0), 0.25, 0.0).astype(BF16)
    rows = MEL_ROWS
    wide = pre_two.shape[1]
    frame_dev = wide - RIM
    usable = masks[0:1]
    share = share_of(devices, chan)
    holders = chan // share

    def every(n):
        return got[pl.ds(n, devices, stride=SECOND), :]

    beside = every(SECOND - 1)[:holders]
    lane = iota((holders, RIM), 1)
    many = rows // 2
    up[0 : many * chan] = dot(own_rows[...], spread)
    for n in range(share):
        first = n * holders
        beyond[first : first + holders, :] = every(3 + n)[:holders]
        beyond[chan + first : chan + first + holders, :] = every(3 + share + n)[:holders]
        for r in range(many + 2):
            at = many * n + (r if r < many else 32 + many - 1 if r == many else 64)
            left, right_of = beside[:, at : at + 1], beside[:, at + 16 : at + 17]
            side = jnp.where(lane >= RIM - 2, 0.25 * left, jnp.where(lane < 2, 0.25 * right_of, 0.0))
            sides[r * chan + first : r * chan + first + holders, :] = side
    up[many * chan :] = dot(beyond[...].astype(BF16), spread)
    total = masks[3:4, 0:1]
    sums = jnp.sum(every(0) + every(1) + every(2), axis=0, keepdims=True)
    mean = to_column(sums, chan) / total
    inv = lax.rsqrt(to_column(sums, chan, chan) / total - mean * mean + 1e-05)
    lane = iota((chan, 128), 1)
    scale = 0.5 * to_column(params[2:3], chan) * inv
    shift = 0.5 * to_column(params[3:4], chan) - mean * scale
    columns = jnp.zeros((chan, 128), F32)
    for n, column in enumerate((mean, inv, scale, shift)):
        columns = jnp.where(lane == n, column, columns)
    stats[0:chan] = columns
    stats[chan : chan + 8] = jnp.broadcast_to(to_lanes(inv), (8, 128))
    shift = jnp.broadcast_to(shift, (chan, wide))
    scale = jnp.broadcast_to(scale, (chan, wide))
    mean = jnp.broadcast_to(mean, (chan, frame_dev))
    inv = jnp.broadcast_to(inv, (chan, frame_dev))
    first = jnp.zeros((chan, 128), F32)
    second = jnp.zeros((chan, 128), F32)
    own_mask = usable[:, :frame_dev]
    right[3 * chan :] = jnp.ones((16, rows * frame_dev), BF16)
    table = jnp.zeros((9 * chan, 3 * chan + 16), F32)
    for q in list(range(2, rows + 2)) + [0, 1, rows + 2, rows + 3]:
        r = q // 2
        at = slice(q * chan, (q + 1) * chan)
        m = q - 2
        mask = 0.5 * usable if 0 <= m < rows else usable * (0.5 * row_valid(m, rows))
        if q % 2 == 0:
            spot = (r - 1 if 1 <= r <= many else many + (r > 0)) * chan
            upstream = jnp.concatenate([up[spot : spot + chan, :], sides[spot : spot + chan, :]], axis=1)
        pre = pre_two[at, :]
        value, slope = silu_halves(pre * scale + shift)
        g = upstream * slope * mask
        grad[at, :] = g
        if not 0 <= m < rows:
            continue
        g = g[:, :frame_dev]
        normed = (pre[:, :frame_dev] - mean) * inv
        first = first + halves(g * normed)
        second = second + halves(g)
        value = value[:, :frame_dev] * own_mask
        both = value if m % 2 == 0 else both + value
        if m % 2:
            pairs[(r - 1) * chan : r * chan, :] = both
        lanes = slice(m * frame_dev, (m + 1) * frame_dev)
        right[0:chan, lanes] = g.astype(BF16)
        right[chan : 2 * chan, lanes] = normed.astype(BF16)
        right[2 * chan : 3 * chan, lanes] = (g - right[0:chan, lanes].astype(F32)).astype(BF16)
        if m in (5, 11, rows - 1):
            start = m - m % 6
            left = [act[(n + 2) * 3 * chan : (n + 5) * 3 * chan, :frame_dev] for n in range(start, m + 1)]
            lanes = slice(start * frame_dev, (m + 1) * frame_dev)
            table = table + dot(jnp.concatenate(left, axis=1), right[:, lanes], ((1,), (1,)))
    first = jnp.sum(first, axis=1, keepdims=True)
    second = jnp.sum(second, axis=1, keepdims=True)
    totals = to_lanes(first) + to_lanes(second, chan)
    block = payload.shape[0] // devices
    payload[pl.ds(0, devices, stride=block), :] = jnp.broadcast_to(totals, (devices, 128))
    rest = jnp.concatenate([table[:, 2 * chan :], jnp.zeros((9 * chan, chan - 16), F32)], axis=1)
    both = table[:, : 2 * chan] + jnp.where(iota(rest.shape, 1) < chan, rest, 0.0)
    single = rest[:, chan : chan + 1]
    lane = iota((devices, 128), 1)
    constants = jnp.zeros((devices, 128), F32)
    for k in range(block - 2):
        cut, ones = both[k * devices : (k + 1) * devices], single[k * devices : (k + 1) * devices]
        short = devices - cut.shape[0]
        if short:
            cut = jnp.concatenate([cut, jnp.zeros((short, 128), F32)], axis=0)
            ones = jnp.concatenate([ones, jnp.zeros((short, 1), F32)], axis=0)
        payload[pl.ds(1 + k, devices, stride=block), :] = cut
        constants = jnp.where(lane == k, ones, constants)
    payload[pl.ds(block - 1, devices, stride=block), :] = constants


def pool(totals, pairs, out, gain_out, bias_out, temp):
    gain_out[...] = totals[0:1, : gain_out.shape[1]]
    bias_out[...] = totals[0:1, gain_out.shape[1] :]
    chan, rows, half = out.shape[1:]
    to_mean = jnp.where(iota((2 * half, half), 0) >> 1 == iota((2 * half, half), 1), 0.25, 0.0)
    pooled = dot(pairs[...], to_mean, precision=EXACT)
    for r in range(rows):
        temp[pl.ds(r, chan, stride=rows), :] = pooled[r * chan : (r + 1) * chan]
    out[0] = temp[...].reshape(chan, rows, half).astype(BF16)


def backward(recv, pre_two, grad, stats_two, w1, x3, stats, params, masks, wb,
             out, payload, totals, g3, pre_one, g1):
    chan = params.shape[1]
    rows = MEL_ROWS
    wide = pre_two.shape[1]
    frame_dev = wide - RIM
    usable = masks[0:1]
    behind, ahead = (masks[n : n + 1].astype(BF16) for n in (1, 2))
    total = masks[3:4, 0:1]
    devices = payload.shape[0] // 14
    pre_one[...] = dot(w1[2 * chan : (rows + 4) * chan], x3[...])

    received = summed_blocks(recv, devices)
    sums = received[0:1]
    gain_sum, bias_sum = sums[:, :chan], sums[:, chan:]
    totals[...] = jnp.broadcast_to(sums, (8, 128))
    mean, inv = stats_two[0:chan, 0:1], stats_two[0:chan, 1:2]
    factor = to_column(params[2:3], chan) * inv
    gain_part = factor * (to_column(sums, chan) / total * inv)
    bias_part = factor * (to_column(sums, chan, chan) / total) - mean * gain_part
    gain_part = jnp.broadcast_to(gain_part, (chan, wide))
    bias_part = jnp.broadcast_to(bias_part, (chan, wide))
    factor = jnp.broadcast_to(factor, (chan, wide))
    scale = jnp.broadcast_to(stats[chan + 16 :, 0:1], (chan, wide))
    shift = jnp.broadcast_to(stats[chan + 16 :, 1:2], (chan, wide))
    factor_one = jnp.broadcast_to(to_column(params[0:1], chan) * stats[0:chan, 1:2], (chan, wide))
    count = pre_two.shape[0] // chan
    table = jnp.zeros((chan, 128), F32)

    def tap_sums(m):
        part = g1[m * chan : (m + 4) * chan, :]
        high = lax.reduce_precision(part, 8, 7)
        low = (part - high).astype(BF16)
        taps_in = x3[:, :frame_dev]
        products = dot(high.astype(BF16), taps_in, ((1,), (1,))) + dot(low, taps_in, ((1,), (1,)))
        moved = [pltpu.roll(products[k * chan : (k + 1) * chan], 128 - (m + k + 3), 1) for k in range(4)]
        return (moved[0] + moved[1]) + (moved[2] + moved[3])

    for q in range(count):
        at = slice(q * chan, (q + 1) * chan)
        mask = usable if 0 <= q - 2 < rows else usable * row_valid(q - 2, rows)
        low = (factor * grad[at, :] - (bias_part + pre_two[at, :] * gain_part) * mask).astype(BF16)
        base = q * 3 * chan
        g3[base : base + chan, :], g3[base + 2 * chan : base + 3 * chan, :] = shifted_frames(low, behind, ahead)
        g3[base + chan : base + 2 * chan, :] = low
        if q < 3 or q % 2 == 0:
            continue
        start = q - 3
        result = dot(wb[...], g3[start * 3 * chan : (start + 4) * 3 * chan, :])
        for n in range(2):
            m = start + n - 1
            at = slice((m + 1) * chan, (m + 2) * chan)
            _, slope = silu_halves(pre_one[at, :] * scale + shift)
            mask = 0.5 * usable if 0 <= m < rows else usable * (0.5 * row_valid(m, rows))
            value = result[n * chan : (n + 1) * chan] * slope * mask
            out[at, :] = (value * factor_one).astype(BF16)
            if not 0 <= m < rows:
                continue
            g1[m * chan : (m + 1) * chan, :] = value[:, :frame_dev]
            if m % 4 == 3 and m > 3:
                table = table + tap_sums(m - 7)
    table = table + tap_sums(rows - 4)
    tap = iota((16, 128), 0)
    lane = iota((16, 128), 1)
    i = (tap * 11) >> 5
    select = ((lane == BAND * (tap - 3 * i) + i) & (tap < 9)) | ((lane == 3 * BAND) & (tap == 9))
    rows10 = dot(select.astype(F32), table, ((1,), (1,)), EXACT)
    share = received.shape[0] - 2
    mine = received[1 : share + 1]
    single = to_column(received[share + 1 :], share)
    factor_l = params[2:3] * stats_two[chan : chan + 1, :chan]
    mine = mine[:, :chan] - (bias_sum * single + gain_sum * mine[:, chan:]) / total
    mine = factor_l * mine
    lower = -(-share // 2)
    mine = jnp.concatenate([mine] + [jnp.zeros((2 * lower - share, chan), F32)] * (share % 2), axis=0)
    mine = jnp.concatenate([mine[:lower], mine[lower:]], axis=1)
    if lower < 9:
        mine = jnp.concatenate([mine, jnp.zeros((9 - lower, 128), F32)], axis=0)
    sums = jnp.concatenate([rows10[0:5], rows10[5:10]], axis=1)
    block = jnp.concatenate([sums, mine], axis=0)
    block = jnp.concatenate([block] * 4, axis=0)
    for d in range(0, devices, 4):
        payload[14 * d : 14 * (d + 4), :] = block


def transposed(low, w1, x3, stats, masks, ws_hbm, first, normed, ws, pre_one, sem):
    load = pltpu.make_async_copy(ws_hbm, ws, sem)
    load.start()
    chan = low.shape[0] // (MEL_ROWS + 2)
    wide = low.shape[1]
    pre_one[...] = dot(w1[2 * chan : (MEL_ROWS + 4) * chan], x3[...])
    mean = jnp.broadcast_to(stats[0:chan, 0:1], (chan, wide))
    inv = jnp.broadcast_to(stats[0:chan, 1:2], (chan, wide))
    for q in range(MEL_ROWS + 2):
        at = slice(q * chan, (q + 1) * chan)
        mask = masks[0:1] * row_valid(q - 1, MEL_ROWS)
        normed[at, :] = ((pre_one[at, :] - mean) * inv * mask).astype(BF16)
    load.wait()
    first[...] = dot(ws[...], low[...])


def finish(recv, features, stats, k1t, first, normed, ws, params, masks,
           spec_hbm, kernel_one_hbm, kernel_two_hbm, gain_hbm, bias_hbm,
           table, spec_grad, kernel_one, kernel_two, gain_out, bias_out, sems):
    chan = params.shape[1]
    rows = MEL_ROWS
    wide = normed.shape[1]
    frame_dev = wide - RIM
    usable, behind, ahead = (masks[n : n + 1] for n in range(3))
    total = masks[3:4, 0:1]
    gain = params[0:1]
    count = recv.shape[0] // 14
    share = -(-9 * chan // count)
    lower = -(-share // 2)
    left = [recv[pl.ds(5 + p, count, stride=14), :] for p in range(lower)]
    whole = jnp.concatenate([v[:, :chan] for v in left] + [v[:, chan:] for v in left], axis=0)
    for t in range(9):
        kernel_two[t] = whole[t * chan : (t + 1) * chan].T
    stores = [pltpu.make_async_copy(kernel_two, kernel_two_hbm, sems.at[3])]
    stores[0].start()
    sums = summed_blocks(recv, count)[0:5]
    ten = jnp.concatenate([sums[:, :chan], sums[:, chan:]], axis=0)
    bias_sum = ten[9:10]
    mean_l, inv_l = stats[chan : chan + 1, :chan], stats[chan + 8 : chan + 9, :chan]
    ten = ten - features[1:2, 0:1] * bias_sum
    k = k1t[0:9]
    gain_sum = inv_l * (jnp.sum(k * ten[0:9], axis=0, keepdims=True) - mean_l * bias_sum)
    gain_out[...] = gain_sum
    bias_out[...] = bias_sum
    for n, (source, target) in enumerate(((gain_out, gain_hbm), (bias_out, bias_hbm))):
        stores.append(pltpu.make_async_copy(source, target, sems.at[n]))
        stores[-1].start()
    factor_l = gain * inv_l
    scale = factor_l * gain_sum / total
    scale = jnp.concatenate([scale, scale], axis=1)
    scale = jnp.concatenate([scale] * ((rows + 2) // 2), axis=1)
    taps = first[...] - dot((ws[...].astype(F32) * scale).astype(BF16), normed[...])
    for part in range(wide // 128):
        table[part] = taps[:, 128 * part : 128 * (part + 1)]
    moved = [
        jnp.concatenate([table[part, pl.ds(b, rows, stride=8), :] for part in range(wide // 128)], axis=1)
        for b in range(3)
    ]
    constant = jnp.sum(k * (factor_l * bias_sum / total), axis=1, keepdims=True)
    for a in range(3):
        row = iota((rows, 1), 0) + (a - 1) + lax.axis_index("mel") * rows
        valid = ((row >= 0) & (row < lax.axis_size("mel") * rows)).astype(F32) * usable
        for b in range(3):
            t = 3 * (2 - a) + 2 - b
            moved[b] = moved[b] - constant[t : t + 1] * valid
    result = pltpu.roll(moved[0], 1, 1) * behind + moved[1] + pltpu.roll(moved[2], wide - 1, 1) * ahead
    spec_grad[0] = (result * usable)[:, :frame_dev]
    stores.append(pltpu.make_async_copy(spec_grad, spec_hbm, sems.at[2]))
    stores[-1].start()
    row = features[0:1, :]
    lane = iota((1, 128), 1)
    gram = jnp.concatenate(
        [jnp.where(lane < 9, pltpu.roll(row, 128 - 9 * t, 1) if t else row, 0.0) for t in range(9)]
        + [jnp.zeros((7, 128), F32)],
        axis=0,
    )
    single = to_column(row, 16, 81)[0:9]
    k_rows = jnp.concatenate([k1t[...], jnp.zeros((112, chan), F32)], axis=0)
    normed_taps = inv_l * (dot(gram, k_rows, precision=EXACT)[0:9] - single * mean_l)
    grad_taps = factor_l * (ten[0:9] - (bias_sum * single + gain_sum * normed_taps) / total)
    for i in range(3):
        kernel_one[i] = grad_taps[3 * i : 3 * i + 3]
    stores.append(pltpu.make_async_copy(kernel_one, kernel_one_hbm, sems.at[4]))
    stores[-1].start()
    for store in stores:
        store.wait()


def run(kernel, outs, scratch, *args, hbm=0, apart=(), flops=10**8, size=4 * 10**6):
    vmem = pl.BlockSpec(memory_space=pltpu.VMEM)
    devices = lax.axis_size("mel") * lax.axis_size("tm")
    specs = []
    args = list(args)
    for n, a in enumerate(args):
        if hbm and n >= len(args) - hbm:
            specs.append(pl.BlockSpec(memory_space=pltpu.HBM))
            args[n] = pltpu.with_memory_space_constraint(a, pltpu.HBM)
        else:
            specs.append(vmem)
            args[n] = pltpu.with_memory_space_constraint(a, pltpu.VMEM)
    return pl.pallas_call(
        kernel,
        out_shape=outs,
        in_specs=specs,
        out_specs=[pl.BlockSpec(memory_space=pltpu.HBM) if n in apart else vmem for n in range(len(outs))],
        scratch_shapes=scratch,
        compiler_params=pltpu.CompilerParams(vmem_limit_bytes=(29 + devices // 32) * 2**20),
        cost_estimate=pl.CostEstimate(flops=flops, bytes_accessed=size, transcendentals=0),
    )(*args)


def shape(dims, dtype=F32):
    return jax.ShapeDtypeStruct(dims, dtype)


def kept(dims, dtype=F32):
    return pltpu.VMEM(dims, dtype)


def far(dims, dtype=F32):
    return pltpu.HBM(dims, dtype)


def exchange(blocks, axes=AXES):
    return lax.all_to_all(blocks, axes, 0, 0, tiled=True)


def exchange_rows(rows, axes=AXES):
    return exchange(rows[:, None, :], axes)[:, 0, :]


def shards(spectrum, clip_bounds, kernel_one, gain_one, bias_one, kernel_two, gain_two, bias_two, pooled_grad):
    _, rows, frame_dev = spectrum.shape
    chan = kernel_two.shape[0]
    n_mel, n_tm = lax.axis_size("mel"), lax.axis_size("tm")
    devices = n_mel * n_tm
    half = frame_dev // 2
    wide = frame_dev + RIM
    mels = n_mel * rows

    packed, own, spec, masks = run(
        pack,
        [
            kept((devices, FIRST, 128), BF16),
            kept(pooled_grad.shape, BF16),
            kept(spectrum.shape, BF16),
            kept((8, wide)),
        ],
        [
            pltpu.SMEM(clip_bounds.shape, jnp.int32),
            pltpu.VMEM((2 * chan, half), F32),
            pltpu.VMEM((devices * FIRST, 128), F32),
            pltpu.SemaphoreType.DMA((3,)),
        ],
        spectrum,
        pooled_grad,
        clip_bounds,
        hbm=3,
    )
    recv = exchange(packed)
    ext = rows + 6
    span = 4 * 3 * chan
    wf, wb, w1, ws, pairs, singles, k1t, params, all_masks, edge_masks, twice, own_rows = run(
        weights,
        [
            kept((2 * chan, span), BF16),
            kept((2 * chan, span), BF16),
            kept((ext * chan, 128), BF16),
            far((rows * 8, (rows + 2) * chan), BF16),
            kept((chan, 128)),
            kept((chan, 128)),
            kept((16, chan)),
            kept((8, chan)),
            kept((3 * n_tm, frame_dev)),
            kept((n_tm * 8, 128)),
            kept((128, 128)),
            kept((chan * rows // 2, half), BF16),
        ],
        [
            pltpu.VMEM((9, chan, chan), BF16),
            pltpu.VMEM((3, 3, chan), BF16),
            pltpu.VMEM((4, 1, chan), F32),
            pltpu.SMEM(clip_bounds.shape, jnp.int32),
            pltpu.VMEM((rows * 8, (rows + 2) * chan), BF16),
            pltpu.VMEM((chan * rows // 2, half), F32),
            pltpu.SemaphoreType.DMA((8,)),
        ],
        own,
        clip_bounds,
        jnp.transpose(kernel_two, (2, 3, 0, 1)).reshape(9, chan, chan),
        jnp.transpose(kernel_one, (1, 2, 0)),
        gain_one[None],
        bias_one[None],
        gain_two[None],
        bias_two[None],
        hbm=7,
        apart=(3,),
    )
    pre_two, payload, act, x3, stats_one, features = run(
        forward_one,
        [
            kept(((rows + 4) * chan, wide)),
            kept((devices, SECOND, 128), BF16),
            kept((ext * 3 * chan, wide), BF16),
            kept((128, wide), BF16),
            kept((2 * chan + 16, 128)),
            kept((8, 128)),
        ],
        [
            pltpu.VMEM((ext * chan, wide), F32),
            pltpu.VMEM((devices * FIRST, 128), F32),
            pltpu.VMEM((n_tm * 8, 128), F32),
            pltpu.VMEM((mels + 8, RIM), F32),
            pltpu.VMEM((devices * SECOND, 128), F32),
        ],
        recv,
        spec,
        pairs,
        singles,
        twice,
        w1,
        wf,
        params,
        masks,
        all_masks,
        edge_masks,
    )
    recv = exchange(payload)
    grad, payload, row_pairs, stats_two = run(
        backward_scaled,
        [
            kept(((rows + 4) * chan, wide)),
            kept((devices * sum_rows(devices, 9 * chan), 128)),
            kept((rows // 2 * chan, frame_dev)),
            kept((chan + 8, 128)),
        ],
        [
            pltpu.VMEM(((rows // 2 + 2) * chan, RIM), F32),
            pltpu.VMEM(((rows // 2 + 2) * chan, frame_dev), F32),
            pltpu.VMEM((3 * chan + 16, rows * frame_dev), BF16),
            pltpu.VMEM((devices * SECOND, 128), F32),
            pltpu.VMEM((2 * chan, half), F32),
        ],
        recv,
        pre_two,
        act,
        own_rows,
        params,
        masks,
    )
    recv = exchange_rows(payload)
    low, payload, totals = run(
        backward,
        [
            kept(((rows + 2) * chan, wide), BF16),
            kept((devices * 14, 128)),
            kept((8, 128)),
        ],
        [
            pltpu.VMEM(((rows + 4) * 3 * chan, wide), BF16),
            pltpu.VMEM(((rows + 2) * chan, wide), F32),
            pltpu.VMEM((rows * chan, frame_dev), F32),
        ],
        recv,
        pre_two,
        grad,
        stats_two,
        w1,
        x3,
        stats_one,
        params,
        masks,
        wb,
    )
    recv = exchange_rows(payload)
    pooled, gain_two_grad, bias_two_grad = run(
        pool,
        [shape((1, chan, rows // 2, half), BF16), shape((1, chan)), shape((1, chan))],
        [
            pltpu.VMEM((rows // 2 * chan, 128), F32),
        ],
        totals,
        row_pairs,
    )
    first, normed, ws = run(
        transposed,
        [
            kept((rows * 8, wide)),
            kept(((rows + 2) * chan, wide), BF16),
            kept((rows * 8, (rows + 2) * chan), BF16),
        ],
        [pltpu.VMEM(((rows + 2) * chan, wide), F32), pltpu.SemaphoreType.DMA],
        low,
        w1,
        x3,
        stats_one,
        masks,
        ws,
        hbm=1,
    )
    spec_grad, kernel_one_grad, kernel_two_grad, gain_one_grad, bias_one_grad = run(
        finish,
        [
            shape((1, rows, frame_dev)),
            shape((3, 3, chan)),
            shape((9, chan, chan)),
            shape((1, chan)),
            shape((1, chan)),
        ],
        [
            pltpu.VMEM((3, rows * 8, 128), F32),
            pltpu.VMEM((1, rows, frame_dev), F32),
            pltpu.VMEM((3, 3, chan), F32),
            pltpu.VMEM((9, chan, chan), F32),
            pltpu.VMEM((1, chan), F32),
            pltpu.VMEM((1, chan), F32),
            pltpu.SemaphoreType.DMA((5,)),
        ],
        recv,
        features,
        stats_one,
        k1t,
        first,
        normed,
        ws,
        params,
        masks,
        apart=range(5),
    )
    kernel_two_grad = jnp.transpose(kernel_two_grad.reshape(3, 3, chan, chan), (2, 3, 0, 1))
    return (
        pooled,
        spec_grad,
        jnp.transpose(kernel_one_grad, (2, 0, 1)),
        gain_one_grad[0],
        bias_one_grad[0],
        kernel_two_grad,
        gain_two_grad[0],
        bias_two_grad[0],
    )


def solution(mesh):
    return jax.shard_map(
        shards,
        mesh=mesh,
        in_specs=(
            P(None, "mel", "tm"),
            P(),
            P(),
            P(),
            P(),
            P(),
            P(),
            P(),
            P(None, None, "mel", "tm"),
        ),
        out_specs=(P(None, None, "mel", "tm"), P(None, "mel", "tm"), P(), P(), P(), P(), P(), P()),
        check_vma=False,
    )
```

```python
import math

import jax
import jax.numpy as jnp
from jax import lax
from jax.experimental import pallas as pl
from jax.experimental.pallas import tpu as pltpu
from jax.sharding import PartitionSpec as P

F32 = jnp.float32
BF16 = jnp.bfloat16
AXES = ("mel", "tm")
EXACT = lax.Precision.HIGHEST
RIM = 128
BAND = 24
MEL_ROWS = 16
FIRST = 24
SUMS, EDGES, COLUMNS = 16, 19, 23
SIDE = 96
SECOND = 8


def iota(shape, dim):
    return lax.broadcasted_iota(jnp.int32, shape, dim)


def dot(a, b, over=((1,), (0,)), precision=None):
    return lax.dot_general(a, b, (over, ((), ())), precision=precision, preferred_element_type=F32)


def to_column(lanes, count, start=0):
    shape = (count, lanes.shape[1])
    return jnp.sum(jnp.where(iota(shape, 1) == iota(shape, 0) + start, lanes, 0.0), axis=1, keepdims=True)


def to_lanes(column, start=0, width=128):
    shape = (column.shape[0], width)
    return jnp.sum(jnp.where(iota(shape, 1) == iota(shape, 0) + start, column, 0.0), axis=0, keepdims=True)


def halves(v):
    total = v[:, :128]
    for n in range(128, v.shape[1], 128):
        total = total + v[:, n : n + 128]
    return total


def frame_masks(bounds, frames):
    last = bounds.shape[1] - 1

    def living(f):
        return (f >= 0) & (f < bounds[0, last])

    def paired(f):
        both = living(f) & living(f + 1)
        for k in range(1, last):
            both = both & (f + 1 != bounds[0, k])
        return both

    return tuple(m.astype(F32) for m in (living(frames), paired(frames - 1), paired(frames)))


def row_valid(row, rows):
    mel = lax.axis_index("mel") * rows + row
    return ((mel >= 0) & (mel < lax.axis_size("mel") * rows)).astype(F32)


def start_all(*pairs, sems):
    copies = [pltpu.make_async_copy(src, dst, sems.at[n]) for n, (src, dst) in enumerate(pairs)]
    for copy in copies:
        copy.start()
    return copies


def wait_all(copies):
    for copy in copies:
        copy.wait()


def shifted_frames(value, behind, ahead):
    wide = value.shape[1]
    return pltpu.roll(value, 1, 1) * behind, pltpu.roll(value, wide - 1, 1) * ahead


def three_parts(v):
    high = lax.reduce_precision(v, 8, 7)
    mid = lax.reduce_precision(v - high, 8, 7)
    return high, mid, v - high - mid


def share_of(devices, chan):
    return -(-chan // devices)


def pack(spec_hbm, grad_hbm, bounds_hbm, out, own, spec, masks, bounds, edges, rows_out, sems):
    copies = start_all((bounds_hbm, bounds), (spec_hbm, spec), (grad_hbm, own), sems=sems)
    copies[0].wait()
    wide = masks.shape[1]
    frame_dev = wide - RIM
    devices = out.shape[0]
    rows = MEL_ROWS
    lane = iota((1, wide), 1)
    frames = lax.axis_index("tm") * frame_dev + jnp.where(lane < frame_dev + RIM // 2, lane, lane - wide)
    last = bounds.shape[1] - 1
    pixels = (bounds[0, last] * (lax.axis_size("mel") * rows)).astype(F32)
    found = frame_masks(bounds, frames)
    masks[...] = jnp.concatenate(
        list(found) + [jnp.full((1, wide), 1.0) * pixels, jnp.zeros((4, wide), F32)], axis=0
    )
    usable, behind, ahead = (m[:, :frame_dev] for m in found)
    copies[1].wait()
    x = spec[0].astype(F32) * usable
    lane = iota((1, frame_dev), 1)
    row = iota((rows, 1), 0)
    inner = jnp.where((lane > 0) & (lane < frame_dev - 1), usable, 0.0)
    number = (rows - 2) * jnp.sum(inner, axis=1, keepdims=True)
    inner = inner * ((row > 0) & (row < rows - 1)).astype(F32)
    centre = jnp.sum(jnp.sum(x, axis=0, keepdims=True), axis=1, keepdims=True)
    centre = centre / (rows * jnp.maximum(jnp.sum(usable, axis=1, keepdims=True), 1.0))
    centre = lax.reduce_precision(centre, 8, 7)
    shifted = [pltpu.roll(x, 1, 1) * behind, x, pltpu.roll(x, frame_dev - 1, 1) * ahead]
    taps = [pltpu.roll(v, (1 - i) % rows, 0) if i != 1 else v for i in range(3) for v in shifted]
    features = feature_rows(centre, (taps, inner))
    lane = iota((1, 128), 1)
    features = jnp.where(lane == 90, centre, jnp.where(lane == 91, number, features))
    pick = iota((8, frame_dev), 0)
    column = jnp.where(pick < 4, pick, frame_dev - 8 + pick)
    strip = dot((iota((8, frame_dev), 1) == column).astype(BF16), x.astype(BF16), ((1,), (1,)))
    lane = iota((8, 128), 1)
    repeat = (iota((rows, 128), 1) % rows == iota((rows, 128), 0)).astype(BF16)
    strip = jnp.where(lane // rows == iota((8, 128), 0), dot(strip.astype(BF16), repeat), 0.0)
    strip = jnp.sum(strip, axis=0, keepdims=True)

    def put(n, value):
        rows_out[pl.ds(n, devices, stride=FIRST), :] = jnp.broadcast_to(value, (devices, 128))

    near = jnp.concatenate([x[0:4], x[rows - 4 :]], axis=0)
    near = jnp.concatenate([near[:, :128], near[:, 128:]], axis=0)
    for d in range(devices):
        rows_out[FIRST * d : FIRST * d + 16, :] = near
    put(COLUMNS, strip)
    copies[2].wait()
    _, chan, many, half = own.shape
    share = share_of(devices, chan)
    holders = chan // share
    g = own[0].astype(F32)
    edges[0:chan] = g[:, 0, :]
    edges[chan:] = g[:, many - 1, :]

    def spread_out(v):
        if holders < devices:
            v = jnp.concatenate([v, jnp.zeros((devices - holders, 128), F32)], axis=0)
        return v

    for n in range(share):
        put(EDGES + n, spread_out(edges[n * holders : (n + 1) * holders, :]))
        put(EDGES + share + n, spread_out(edges[chan + n * holders : chan + (n + 1) * holders, :]))
    for n in range(2 * share, COLUMNS - EDGES):
        put(EDGES + n, jnp.zeros((1, 128), F32))
    end = iota((8, half), 0)
    at = iota((8, half), 1)
    ends = ((end == 0) & (at == 0)) | ((end == 1) & (at == half - 1))
    columns = dot(ends.astype(BF16), g.reshape(chan * many, half).astype(BF16), ((1,), (1,)))
    group = 128 // many
    source = iota((128, 128), 0)
    lane = iota((group, 128), 1)
    mine = lane // many == iota((group, 128), 0)
    parts = three_parts(features)
    for n in range(2):
        side = jnp.zeros((holders, 128), F32)
        for m in range(share):
            move = (iota((128, 128), 1) == SIDE + many * m + source % many).astype(BF16)
            first = m * holders * many // 128
            block = [columns[n : n + 1, 128 * q : 128 * (q + 1)] for q in range(first, first + holders * many // 128)]
            block = jnp.concatenate([jnp.where(mine, v, 0.0) for v in block], axis=0)
            side = side + dot(block.astype(BF16), move)
        put(SUMS + n, spread_out(side) + parts[n])
    put(SUMS + 2, parts[2])
    out[...] = rows_out[...].reshape(out.shape).astype(BF16)


def weights(own, bounds_hbm, k2_hbm, k1_hbm, gain_one_hbm, bias_one_hbm, gain_two_hbm, bias_two_hbm,
            wf, wb, w1, ws_hbm, pairs, singles, k1t, params, all_masks, edge_masks, twice, own_rows,
            k2, k1, vectors, bounds, ws, temp, sems):
    loads = start_all(
        (bounds_hbm, bounds),
        (k2_hbm, k2),
        (k1_hbm, k1),
        (gain_one_hbm, vectors.at[0]),
        (bias_one_hbm, vectors.at[1]),
        (gain_two_hbm, vectors.at[2]),
        (bias_two_hbm, vectors.at[3]),
        sems=sems,
    )
    _, many, count, half = own.shape
    temp[...] = own[0].astype(F32).reshape(many * count, half)
    for r in range(count):
        own_rows[r * many : (r + 1) * many] = temp[pl.ds(r, many, stride=count), :].astype(BF16)
    wait_all(loads)
    chan = k2.shape[1]
    span = wf.shape[1]
    taps = [k2[t].astype(F32) for t in range(9)]
    rest = jnp.zeros((chan, span - 9 * chan), F32)
    forward = jnp.concatenate(taps + [rest], axis=1)
    backward = jnp.concatenate([taps[8 - t].T for t in range(9)] + [rest], axis=1)
    for r in range(wb.shape[0] // chan):
        at = slice(r * chan, (r + 1) * chan)
        wb[at] = (pltpu.roll(backward, 3 * chan * r, 1) if r else backward).astype(BF16)
    full = jnp.concatenate([k1[n].astype(F32) for n in range(3)] + [jnp.zeros((7, chan), F32)], axis=0)
    low = [
        jnp.concatenate([full[3 * (2 - a) + 2 - b : 3 * (2 - a) + 3 - b] for a in range(3)], axis=1)
        for b in range(3)
    ]
    base = jnp.concatenate(low + [jnp.zeros((5, 3 * chan), F32)], axis=0)
    base = jnp.concatenate([base, jnp.zeros((8, ws.shape[1] - 3 * chan), F32)], axis=1)
    for m in range(ws.shape[0] // 8):
        ws[8 * m : 8 * m + 8] = (pltpu.roll(base, chan * m, 1) if m else base).astype(BF16)
    store_ws = pltpu.make_async_copy(ws, ws_hbm, sems.at[7])
    store_ws.start()
    count, frame_dev = all_masks.shape[0] // 3, all_masks.shape[1]
    frames = iota((count, frame_dev), 0) * frame_dev + iota((count, frame_dev), 1)
    for n, mask in enumerate(frame_masks(bounds, frames)):
        all_masks[n * count : (n + 1) * count] = mask
    q = iota(edge_masks.shape, 0)
    lane = iota(edge_masks.shape, 1)
    k = q % 8
    frames = (q // 8) * frame_dev + jnp.where(k < 4, k, k + frame_dev - 8)
    living, behind, ahead = frame_masks(bounds, frames)
    living = jnp.where((k == 0) | (k == 7), living, 0.0)
    edge_masks[...] = jnp.where(lane == 0, living, jnp.where(lane == 1, behind, jnp.where(lane == 2, ahead, 0.0)))
    params[...] = jnp.concatenate(
        [vectors[n] for n in range(4)] + [jnp.zeros((4, chan), F32)], axis=0
    )
    tap = iota((16, 128), 0)
    lane = iota((16, 128), 1)
    i = (tap * 11) >> 5
    ninth = (lane * 57) >> 9
    to_band = (lane == BAND * (tap - 3 * i) + i) & (tap < 9)
    to_left = (ninth == tap) & (tap < 9)
    to_right = (lane - 9 * ninth == tap) & (lane < 81)
    to_single = (lane == 81 + tap) & (tap < 9)
    source = iota((128, 128), 0) - 81
    lane = iota((128, 128), 1)
    ninth = (lane * 57) >> 9
    inside = (source >= 0) & (source < 9) & (lane < 81)
    twice[...] = jnp.where(inside, (source == ninth).astype(F32) + (source == lane - 9 * ninth).astype(F32), 0.0)
    for r in range(wf.shape[0] // chan):
        at = slice(r * chan, (r + 1) * chan)
        wf[at] = (pltpu.roll(forward, 3 * chan * r, 1) if r else forward).astype(BF16)
    k1t[...] = full
    k = full.astype(BF16)
    lanes = [dot(k, select.astype(BF16), ((0,), (0,))) for select in (to_band, to_left, to_right, to_single)]
    pairs[...] = lanes[1] * lanes[2]
    singles[...] = lanes[3]
    for m in range(w1.shape[0] // chan):
        w1[m * chan : (m + 1) * chan] = (pltpu.roll(lanes[0], m, 1) if m else lanes[0]).astype(BF16)
    store_ws.wait()


def feature_rows(centre, *parts):
    def folded(v):
        return jnp.sum(halves(v), axis=0, keepdims=True)

    rows = [jnp.zeros((1, 128), F32)] * 96
    for taps, weight in parts:
        z = [tap - centre for tap in taps]
        for s in range(9):
            left = z[s] * weight
            rows[81 + s] = rows[81 + s] + folded(left)
            for t in range(s, 9):
                rows[9 * s + t] = rows[9 * t + s] = rows[9 * s + t] + folded(left * z[t])
    return to_lanes(jnp.sum(jnp.concatenate(rows, axis=0), axis=1, keepdims=True))


def summed_blocks(ref, devices):
    block = ref.shape[0] // devices
    period = 8 // math.gcd(block, 8)
    step = period * block
    total = ref[0:step, :]
    for at in range(step, ref.shape[0], step):
        total = total + ref[at : at + step, :]
    result = total[0:block]
    for n in range(1, period):
        result = result + total[n * block : (n + 1) * block]
    return result


def moved_rows(v, step):
    if step == 0:
        return v
    count = v.shape[0]
    if abs(step) >= count:
        return jnp.zeros_like(v)
    zero = jnp.zeros((abs(step), v.shape[1]), v.dtype)
    if step > 0:
        return jnp.concatenate([zero, v[: count - step]], axis=0)
    return jnp.concatenate([v[-step:], zero], axis=0)


def silu_halves(h):
    t = jnp.tanh(h)
    one = 1.0 + t
    return h * one, one * (1.0 + h * (1.0 - t))


def forward_one(recv, spec, pairs, singles, twice, w1, wf, params, masks, all_masks, edge_masks,
                pre_two, payload, act, x3, stats, features_out, pre_one, got, strips, halo, rows_out):
    devices = recv.shape[0]
    n_mel, count = lax.axis_size("mel"), lax.axis_size("tm")
    rows = MEL_ROWS
    mels = n_mel * rows
    wide = masks.shape[1]
    frame_dev = wide - RIM
    chan = params.shape[1]
    me_m, me_t = lax.axis_index("mel"), lax.axis_index("tm")
    usable, behind, ahead = (masks[n : n + 1] for n in range(3))
    total = masks[3:4, 0:1]
    got[...] = recv[...].astype(F32).reshape(devices * FIRST, 128)

    def every(n):
        return got[pl.ds(n, devices, stride=FIRST), :]

    lane = iota((count, 128), 1)
    bands = [got[pl.ds(FIRST * k * count + COLUMNS, count, stride=FIRST), :] for k in range(n_mel)]
    for c in range(8):
        column = jnp.zeros((count, 128), F32)
        for k, band in enumerate(bands):
            part = jnp.where(lane // rows == c, band, 0.0)
            column = column + (pltpu.roll(part, rows * (k - c) % 128, 1) if k != c else part)
        strips[pl.ds(c, count, stride=8), :] = column
    at = pl.multiple_of(FIRST * (jnp.maximum(me_m - 1, 0) * count + me_t), 8)
    above = got[pl.ds(at, 16), :] * (me_m > 0).astype(F32)
    at = pl.multiple_of(FIRST * (jnp.minimum(me_m + 1, n_mel - 1) * count + me_t), 8)
    below = got[pl.ds(at, 16), :] * (me_m < n_mel - 1).astype(F32)
    above = jnp.concatenate([above[4:8], above[12:16]], axis=1)
    below = jnp.concatenate([below[0:4], below[8:12]], axis=1)
    own = spec[0].astype(F32) * usable[:, :frame_dev]
    at = pl.multiple_of(8 * jnp.minimum(me_t + 1, count - 1), 8)
    after = strips[pl.ds(at, 8), :][:, :mels] * (me_t + 1 < count).astype(F32)
    at = pl.multiple_of(8 * jnp.maximum(me_t - 1, 0), 8)
    before = strips[pl.ds(at, 8), :][:, :mels] * (me_t > 0).astype(F32)
    sides = jnp.concatenate([after[0:4], before[4:8], jnp.zeros((8, mels), F32)], axis=0).astype(BF16)
    side = iota((16, RIM), 0)
    place = iota((16, RIM), 1) == jnp.where(side < 4, side, jnp.where(side < 8, side + RIM - 8, -1))
    halo[0:8] = jnp.zeros((8, RIM), F32)
    halo[mels : mels + 8] = jnp.zeros((8, RIM), F32)
    halo[4 : mels + 4] = dot(sides, place.astype(BF16), ((0,), (0,)))
    rim = halo[pl.ds(pl.multiple_of(me_m * rows, 8), BAND), :]
    near = jnp.concatenate([jnp.concatenate([above, own, below], axis=0), rim], axis=1)
    x3[...] = jnp.concatenate(
        [
            pltpu.roll(near, 1, 1) * behind,
            near,
            pltpu.roll(near, wide - 1, 1) * ahead,
            jnp.broadcast_to(usable, (BAND, wide)),
            jnp.zeros((128 - 4 * BAND, wide), F32),
        ],
        axis=0,
    ).astype(BF16)
    pre_one[...] = dot(w1[...], x3[...])
    lane = iota((1, 128), 1)
    parts = jnp.where(lane < 92, every(SUMS) + every(SUMS + 1) + every(SUMS + 2), 0.0)
    centres, numbers = parts[:, 90:91], parts[:, 91:92]
    centre = jnp.sum(centres * numbers, axis=0, keepdims=True)
    centre = centre / jnp.maximum(jnp.sum(numbers, axis=0, keepdims=True), 1.0)
    delta = centres - centre
    features = jnp.sum(parts + delta * numbers * jnp.where(lane < 81, delta, 1.0), axis=0, keepdims=True)
    moved = jnp.sum(delta * parts, axis=0, keepdims=True)
    def edge_row(k, n):
        first = FIRST * k * count + n
        return jnp.concatenate(
            [got[pl.ds(first, count, stride=FIRST), :], got[pl.ds(first + 8, count, stride=FIRST), :]], axis=1
        )

    edge_rows = [[edge_row(k, n) for n in (0, 1, 6, 7)] for k in range(n_mel)]
    zero = jnp.zeros((count, frame_dev), F32)
    rows_of = [[], [], []]
    for k, (top, second, fore, bottom) in enumerate(edge_rows):
        for n, v in enumerate((edge_rows[k - 1][3] if k else zero, top, second)):
            rows_of[n].append(v)
        for n, v in enumerate((fore, bottom, edge_rows[k + 1][0] if k + 1 < n_mel else zero)):
            rows_of[n].append(v)
    f_usable, f_behind, f_ahead = (all_masks[n * count : (n + 1) * count, :] for n in range(3))
    lane = iota((count, frame_dev), 1)

    def frame_before(v):
        v = pltpu.roll(v, 1, 1)
        return jnp.where(lane == 0, pltpu.roll(v, 1, 0), v) * f_behind

    def frame_after(v):
        v = pltpu.roll(v, frame_dev - 1, 1)
        return jnp.where(lane == frame_dev - 1, pltpu.roll(v, count - 1, 0), v) * f_ahead

    taps = []
    for group in rows_of:
        for move in (frame_before, lambda v: v, frame_after):
            taps.append(jnp.concatenate([move(v) for v in group], axis=1))
    f_usable = jnp.concatenate([f_usable] * (2 * n_mel), axis=1)
    borders = (taps, f_usable)
    edge = strips[...]
    q_usable, q_behind, q_ahead = (edge_masks[:, n : n + 1] for n in range(3))
    lane = iota((count * 8, 128), 1)
    inside = (lane < mels) & (lane % rows != 0) & (lane % rows != rows - 1)
    shifted = [
        pltpu.roll(edge, 1, 0) * q_behind,
        edge,
        pltpu.roll(edge, count * 8 - 1, 0) * q_ahead,
    ]
    taps = [pltpu.roll(v, (1 - i) % 128, 1) if i != 1 else v for i in range(3) for v in shifted]
    features = features + feature_rows(centre, borders, (taps, jnp.where(inside, q_usable, 0.0)))
    features = jnp.where(iota((1, 128), 1) < 90, features, 0.0)
    near_mean = jnp.sum(singles[...] * features, axis=1, keepdims=True) / total
    around = jnp.sum(singles[...], axis=1, keepdims=True)
    square = jnp.sum(pairs[...] * features, axis=1, keepdims=True)
    square = (square + 2.0 * around * jnp.sum(singles[...] * moved, axis=1, keepdims=True)) / total
    inv = lax.rsqrt(square - near_mean * near_mean + 1e-05)
    mean = near_mean + centre * around
    lane = iota((chan, 128), 1)
    stats[0:chan] = jnp.where(lane == 0, mean, jnp.where(lane == 1, inv, 0.0))
    stats[chan : chan + 8] = jnp.broadcast_to(to_lanes(near_mean), (8, 128))
    stats[chan + 8 : chan + 16] = jnp.broadcast_to(to_lanes(inv), (8, 128))
    scale = 0.5 * to_column(params[0:1], chan) * inv
    shift = 0.5 * to_column(params[1:2], chan) - mean * scale
    stats[chan + 16 :] = jnp.where(lane == 0, scale, jnp.where(lane == 1, shift, 0.0))
    scale = jnp.broadcast_to(scale, (chan, wide))
    shift = jnp.broadcast_to(shift, (chan, wide))
    ext = w1.shape[0] // chan
    block, taps = wf.shape
    first = jnp.zeros((chan, 128), F32)
    second = jnp.zeros((chan, 128), F32)
    own_mask = usable[:, :frame_dev]
    low_masks = [m.astype(BF16) for m in (usable, behind, ahead)]
    waiting = None

    def row_sums(g, result, first, second):
        pre_two[g * block : (g + 1) * block] = result
        for q in range(2):
            if 2 <= 2 * g + q < rows + 2:
                p = result[q * chan : (q + 1) * chan, :frame_dev]
                masked = p * own_mask
                first = first + halves(masked)
                second = second + halves(masked * p)
        return first, second

    for r in range(ext):
        value, _ = silu_halves(pre_one[r * chan : (r + 1) * chan, :] * scale + shift)
        if not 0 <= r - 3 < rows:
            value = value * row_valid(r - 3, rows)
        base = r * 3 * chan
        low = value.astype(BF16) * low_masks[0]
        act[base : base + chan, :], act[base + 2 * chan : base + 3 * chan, :] = shifted_frames(low, *low_masks[1:])
        act[base + chan : base + 2 * chan, :] = low
        if r < 3 or r % 2 == 0:
            continue
        g = (r - 3) // 2
        result = dot(wf[...], act[g * 3 * block : g * 3 * block + taps, :])
        if waiting is not None:
            first, second = row_sums(g - 1, waiting, first, second)
        waiting = result
    first, second = row_sums(g, waiting, first, second)
    moved = dot(jnp.broadcast_to(moved, (8, 128)), twice[...], precision=EXACT)[0:1]
    features_out[...] = jnp.concatenate(
        [features + moved, jnp.broadcast_to(centre, (1, 128)), jnp.zeros((6, 128), F32)], axis=0
    )
    share = share_of(devices, chan)

    def put(n, value):
        rows_out[pl.ds(n, devices, stride=SECOND), :] = jnp.broadcast_to(value, (devices, 128))

    for n in range(share):
        put(3 + n, moved_rows(every(EDGES + share + n), count))
        put(3 + share + n, moved_rows(every(EDGES + n), -count))
    for n in range(3 + 2 * share, SECOND - 1):
        put(n, jnp.zeros((1, 128), F32))
    lane = iota((devices, 128), 1)
    tm = iota((devices, 128), 0) % count
    lefts = jnp.where(lane >= SIDE, every(SUMS), 0.0)
    rights = jnp.where(lane >= SIDE, every(SUMS + 1), 0.0)
    beside = jnp.zeros((devices, 128), F32)
    for n, step in enumerate((0, count, -count)):
        one = jnp.where(tm > 0, moved_rows(rights, step + 1), 0.0)
        two = jnp.where(tm < count - 1, moved_rows(lefts, step - 1), 0.0)
        beside = beside + pltpu.roll(one, (32 * n - SIDE) % 128, 1) + pltpu.roll(two, (32 * n + 16 - SIDE) % 128, 1)
    put(SECOND - 1, beside)
    first = jnp.sum(first, axis=1, keepdims=True)
    second = jnp.sum(second, axis=1, keepdims=True)
    for n, part in enumerate(three_parts(to_lanes(first) + to_lanes(second, chan))):
        put(n, part)
    payload[...] = rows_out[...].reshape(payload.shape).astype(BF16)


def sum_rows(devices, taps):
    return -(-taps // devices) + 2


def backward_scaled(recv, pre_two, act, own_rows, params, masks,
                    grad, payload, pairs, stats, sides, up, right, got, beyond):
    devices = recv.shape[0]
    got[...] = recv[...].astype(F32).reshape(devices * SECOND, 128)
    chan = params.shape[1]
    half = own_rows.shape[1]
    lane = iota((half, 2 * half), 1)
    spread = jnp.where(lane >> 1 == iota((half, 2 * half), 0), 0.25, 0.0).astype(BF16)
    rows = MEL_ROWS
    wide = pre_two.shape[1]
    frame_dev = wide - RIM
    usable = masks[0:1]
    share = share_of(devices, chan)
    holders = chan // share

    def every(n):
        return got[pl.ds(n, devices, stride=SECOND), :]

    beside = every(SECOND - 1)[:holders]
    lane = iota((holders, RIM), 1)
    many = rows // 2
    up[0 : many * chan] = dot(own_rows[...], spread)
    for n in range(share):
        first = n * holders
        beyond[first : first + holders, :] = every(3 + n)[:holders]
        beyond[chan + first : chan + first + holders, :] = every(3 + share + n)[:holders]
        for r in range(many + 2):
            at = many * n + (r if r < many else 32 + many - 1 if r == many else 64)
            left, right_of = beside[:, at : at + 1], beside[:, at + 16 : at + 17]
            side = jnp.where(lane >= RIM - 2, 0.25 * left, jnp.where(lane < 2, 0.25 * right_of, 0.0))
            sides[r * chan + first : r * chan + first + holders, :] = side
    up[many * chan :] = dot(beyond[...].astype(BF16), spread)
    total = masks[3:4, 0:1]
    sums = jnp.sum(every(0) + every(1) + every(2), axis=0, keepdims=True)
    mean = to_column(sums, chan) / total
    inv = lax.rsqrt(to_column(sums, chan, chan) / total - mean * mean + 1e-05)
    lane = iota((chan, 128), 1)
    scale = 0.5 * to_column(params[2:3], chan) * inv
    shift = 0.5 * to_column(params[3:4], chan) - mean * scale
    columns = jnp.zeros((chan, 128), F32)
    for n, column in enumerate((mean, inv, scale, shift)):
        columns = jnp.where(lane == n, column, columns)
    stats[0:chan] = columns
    stats[chan : chan + 8] = jnp.broadcast_to(to_lanes(inv), (8, 128))
    shift = jnp.broadcast_to(shift, (chan, wide))
    scale = jnp.broadcast_to(scale, (chan, wide))
    mean = jnp.broadcast_to(mean, (chan, frame_dev))
    inv = jnp.broadcast_to(inv, (chan, frame_dev))
    first = jnp.zeros((chan, 128), F32)
    second = jnp.zeros((chan, 128), F32)
    own_mask = usable[:, :frame_dev]
    right[3 * chan :] = jnp.ones((16, rows * frame_dev), BF16)
    table = jnp.zeros((9 * chan, 3 * chan + 16), F32)
    for q in list(range(2, rows + 2)) + [0, 1, rows + 2, rows + 3]:
        r = q // 2
        at = slice(q * chan, (q + 1) * chan)
        m = q - 2
        mask = 0.5 * usable if 0 <= m < rows else usable * (0.5 * row_valid(m, rows))
        if q % 2 == 0:
            spot = (r - 1 if 1 <= r <= many else many + (r > 0)) * chan
            upstream = jnp.concatenate([up[spot : spot + chan, :], sides[spot : spot + chan, :]], axis=1)
        pre = pre_two[at, :]
        value, slope = silu_halves(pre * scale + shift)
        g = upstream * slope * mask
        grad[at, :] = g
        if not 0 <= m < rows:
            continue
        g = g[:, :frame_dev]
        normed = (pre[:, :frame_dev] - mean) * inv
        first = first + halves(g * normed)
        second = second + halves(g)
        value = value[:, :frame_dev] * own_mask
        both = value if m % 2 == 0 else both + value
        if m % 2:
            pairs[(r - 1) * chan : r * chan, :] = both
        lanes = slice(m * frame_dev, (m + 1) * frame_dev)
        right[0:chan, lanes] = g.astype(BF16)
        right[chan : 2 * chan, lanes] = normed.astype(BF16)
        right[2 * chan : 3 * chan, lanes] = (g - right[0:chan, lanes].astype(F32)).astype(BF16)
        if m in (5, 11, rows - 1):
            start = m - m % 6
            left = [act[(n + 2) * 3 * chan : (n + 5) * 3 * chan, :frame_dev] for n in range(start, m + 1)]
            lanes = slice(start * frame_dev, (m + 1) * frame_dev)
            table = table + dot(jnp.concatenate(left, axis=1), right[:, lanes], ((1,), (1,)))
    first = jnp.sum(first, axis=1, keepdims=True)
    second = jnp.sum(second, axis=1, keepdims=True)
    totals = to_lanes(first) + to_lanes(second, chan)
    block = payload.shape[0] // devices
    payload[pl.ds(0, devices, stride=block), :] = jnp.broadcast_to(totals, (devices, 128))
    rest = jnp.concatenate([table[:, 2 * chan :], jnp.zeros((9 * chan, chan - 16), F32)], axis=1)
    both = table[:, : 2 * chan] + jnp.where(iota(rest.shape, 1) < chan, rest, 0.0)
    single = rest[:, chan : chan + 1]
    lane = iota((devices, 128), 1)
    constants = jnp.zeros((devices, 128), F32)
    for k in range(block - 2):
        cut, ones = both[k * devices : (k + 1) * devices], single[k * devices : (k + 1) * devices]
        short = devices - cut.shape[0]
        if short:
            cut = jnp.concatenate([cut, jnp.zeros((short, 128), F32)], axis=0)
            ones = jnp.concatenate([ones, jnp.zeros((short, 1), F32)], axis=0)
        payload[pl.ds(1 + k, devices, stride=block), :] = cut
        constants = jnp.where(lane == k, ones, constants)
    payload[pl.ds(block - 1, devices, stride=block), :] = constants


def pool(totals, pairs, out, gain_out, bias_out, temp):
    gain_out[...] = totals[0:1, : gain_out.shape[1]]
    bias_out[...] = totals[0:1, gain_out.shape[1] :]
    chan, rows, half = out.shape[1:]
    to_mean = jnp.where(iota((2 * half, half), 0) >> 1 == iota((2 * half, half), 1), 0.25, 0.0)
    pooled = dot(pairs[...], to_mean, precision=EXACT)
    for r in range(rows):
        temp[pl.ds(r, chan, stride=rows), :] = pooled[r * chan : (r + 1) * chan]
    out[0] = temp[...].reshape(chan, rows, half).astype(BF16)


def backward(recv, pre_two, grad, stats_two, w1, x3, stats, params, masks, wb,
             out, payload, totals, g3, pre_one, g1):
    chan = params.shape[1]
    rows = MEL_ROWS
    wide = pre_two.shape[1]
    frame_dev = wide - RIM
    usable = masks[0:1]
    behind, ahead = (masks[n : n + 1].astype(BF16) for n in (1, 2))
    total = masks[3:4, 0:1]
    devices = payload.shape[0] // 14
    pre_one[...] = dot(w1[2 * chan : (rows + 4) * chan], x3[...])

    received = summed_blocks(recv, devices)
    sums = received[0:1]
    gain_sum, bias_sum = sums[:, :chan], sums[:, chan:]
    totals[...] = jnp.broadcast_to(sums, (8, 128))
    mean, inv = stats_two[0:chan, 0:1], stats_two[0:chan, 1:2]
    factor = to_column(params[2:3], chan) * inv
    gain_part = factor * (to_column(sums, chan) / total * inv)
    bias_part = factor * (to_column(sums, chan, chan) / total) - mean * gain_part
    gain_part = jnp.broadcast_to(gain_part, (chan, wide))
    bias_part = jnp.broadcast_to(bias_part, (chan, wide))
    factor = jnp.broadcast_to(factor, (chan, wide))
    scale = jnp.broadcast_to(stats[chan + 16 :, 0:1], (chan, wide))
    shift = jnp.broadcast_to(stats[chan + 16 :, 1:2], (chan, wide))
    factor_one = jnp.broadcast_to(to_column(params[0:1], chan) * stats[0:chan, 1:2], (chan, wide))
    count = pre_two.shape[0] // chan
    table = jnp.zeros((chan, 128), F32)

    waiting = None

    def sloped(start, result):
        for n in range(2):
            m = start + n - 1
            at = slice((m + 1) * chan, (m + 2) * chan)
            _, slope = silu_halves(pre_one[at, :] * scale + shift)
            mask = 0.5 * usable if 0 <= m < rows else usable * (0.5 * row_valid(m, rows))
            value = result[n * chan : (n + 1) * chan] * slope * mask
            out[at, :] = (value * factor_one).astype(BF16)
            if 0 <= m < rows:
                g1[m * chan : (m + 1) * chan, :] = value[:, :frame_dev]

    def tap_sums(m):
        part = g1[m * chan : (m + 4) * chan, :]
        high = lax.reduce_precision(part, 8, 7)
        both = jnp.concatenate([high.astype(BF16), (part - high).astype(BF16)], axis=1)
        taps_in = x3[:, :frame_dev]
        products = dot(both, jnp.concatenate([taps_in, taps_in], axis=1), ((1,), (1,)))
        moved = [pltpu.roll(products[k * chan : (k + 1) * chan], 128 - (m + k + 3), 1) for k in range(4)]
        return (moved[0] + moved[1]) + (moved[2] + moved[3])

    for q in range(count):
        at = slice(q * chan, (q + 1) * chan)
        mask = usable if 0 <= q - 2 < rows else usable * row_valid(q - 2, rows)
        low = (factor * grad[at, :] - (bias_part + pre_two[at, :] * gain_part) * mask).astype(BF16)
        base = q * 3 * chan
        g3[base : base + chan, :], g3[base + 2 * chan : base + 3 * chan, :] = shifted_frames(low, behind, ahead)
        g3[base + chan : base + 2 * chan, :] = low
        if q < 3 or q % 2 == 0:
            continue
        start = q - 3
        result = dot(wb[...], g3[start * 3 * chan : (start + 4) * 3 * chan, :])
        if waiting is not None:
            sloped(start - 2, waiting)
        waiting = result
        if start % 4 == 2 and start > 4:
            table = table + tap_sums(start - 6)
    sloped(rows, waiting)
    table = table + tap_sums(rows - 4)
    tap = iota((16, 128), 0)
    lane = iota((16, 128), 1)
    i = (tap * 11) >> 5
    select = ((lane == BAND * (tap - 3 * i) + i) & (tap < 9)) | ((lane == 3 * BAND) & (tap == 9))
    rows10 = dot(select.astype(F32), table, ((1,), (1,)), EXACT)
    share = received.shape[0] - 2
    mine = received[1 : share + 1]
    single = to_column(received[share + 1 :], share)
    factor_l = params[2:3] * stats_two[chan : chan + 1, :chan]
    mine = mine[:, :chan] - (bias_sum * single + gain_sum * mine[:, chan:]) / total
    mine = factor_l * mine
    lower = -(-share // 2)
    mine = jnp.concatenate([mine] + [jnp.zeros((2 * lower - share, chan), F32)] * (share % 2), axis=0)
    mine = jnp.concatenate([mine[:lower], mine[lower:]], axis=1)
    if lower < 9:
        mine = jnp.concatenate([mine, jnp.zeros((9 - lower, 128), F32)], axis=0)
    sums = jnp.concatenate([rows10[0:5], rows10[5:10]], axis=1)
    block = jnp.concatenate([sums, mine], axis=0)
    block = jnp.concatenate([block] * 4, axis=0)
    for d in range(0, devices, 4):
        payload[14 * d : 14 * (d + 4), :] = block


def transposed(low, w1, x3, stats, masks, ws_hbm, first, normed, ws, pre_one, sem):
    load = pltpu.make_async_copy(ws_hbm, ws, sem)
    load.start()
    chan = low.shape[0] // (MEL_ROWS + 2)
    wide = low.shape[1]
    pre_one[...] = dot(w1[2 * chan : (MEL_ROWS + 4) * chan], x3[...])
    mean = jnp.broadcast_to(stats[0:chan, 0:1], (chan, wide))
    inv = jnp.broadcast_to(stats[0:chan, 1:2], (chan, wide))
    for q in range(MEL_ROWS + 2):
        at = slice(q * chan, (q + 1) * chan)
        mask = masks[0:1] * row_valid(q - 1, MEL_ROWS)
        normed[at, :] = ((pre_one[at, :] - mean) * inv * mask).astype(BF16)
    load.wait()
    first[...] = dot(ws[...], low[...])


def finish(recv, features, stats, k1t, first, normed, ws, params, masks,
           spec_hbm, kernel_one_hbm, kernel_two_hbm, gain_hbm, bias_hbm,
           table, spec_grad, kernel_one, kernel_two, gain_out, bias_out, sems):
    chan = params.shape[1]
    rows = MEL_ROWS
    wide = normed.shape[1]
    frame_dev = wide - RIM
    usable, behind, ahead = (masks[n : n + 1] for n in range(3))
    total = masks[3:4, 0:1]
    gain = params[0:1]
    count = recv.shape[0] // 14
    share = -(-9 * chan // count)
    lower = -(-share // 2)
    left = [recv[pl.ds(5 + p, count, stride=14), :] for p in range(lower)]
    whole = jnp.concatenate([v[:, :chan] for v in left] + [v[:, chan:] for v in left], axis=0)
    for t in range(9):
        kernel_two[t] = whole[t * chan : (t + 1) * chan].T
    stores = [pltpu.make_async_copy(kernel_two, kernel_two_hbm, sems.at[3])]
    stores[0].start()
    sums = summed_blocks(recv, count)[0:5]
    ten = jnp.concatenate([sums[:, :chan], sums[:, chan:]], axis=0)
    bias_sum = ten[9:10]
    mean_l, inv_l = stats[chan : chan + 1, :chan], stats[chan + 8 : chan + 9, :chan]
    ten = ten - features[1:2, 0:1] * bias_sum
    k = k1t[0:9]
    gain_sum = inv_l * (jnp.sum(k * ten[0:9], axis=0, keepdims=True) - mean_l * bias_sum)
    gain_out[...] = gain_sum
    bias_out[...] = bias_sum
    for n, (source, target) in enumerate(((gain_out, gain_hbm), (bias_out, bias_hbm))):
        stores.append(pltpu.make_async_copy(source, target, sems.at[n]))
        stores[-1].start()
    factor_l = gain * inv_l
    scale = factor_l * gain_sum / total
    scale = jnp.concatenate([scale, scale], axis=1)
    scale = jnp.concatenate([scale] * ((rows + 2) // 2), axis=1)
    taps = first[...] - dot((ws[...].astype(F32) * scale).astype(BF16), normed[...])
    for part in range(wide // 128):
        table[part] = taps[:, 128 * part : 128 * (part + 1)]
    moved = [
        jnp.concatenate([table[part, pl.ds(b, rows, stride=8), :] for part in range(wide // 128)], axis=1)
        for b in range(3)
    ]
    constant = jnp.sum(k * (factor_l * bias_sum / total), axis=1, keepdims=True)
    for a in range(3):
        row = iota((rows, 1), 0) + (a - 1) + lax.axis_index("mel") * rows
        valid = ((row >= 0) & (row < lax.axis_size("mel") * rows)).astype(F32) * usable
        for b in range(3):
            t = 3 * (2 - a) + 2 - b
            moved[b] = moved[b] - constant[t : t + 1] * valid
    result = pltpu.roll(moved[0], 1, 1) * behind + moved[1] + pltpu.roll(moved[2], wide - 1, 1) * ahead
    spec_grad[0] = (result * usable)[:, :frame_dev]
    stores.append(pltpu.make_async_copy(spec_grad, spec_hbm, sems.at[2]))
    stores[-1].start()
    row = features[0:1, :]
    lane = iota((1, 128), 1)
    gram = jnp.concatenate(
        [jnp.where(lane < 9, pltpu.roll(row, 128 - 9 * t, 1) if t else row, 0.0) for t in range(9)]
        + [jnp.zeros((7, 128), F32)],
        axis=0,
    )
    single = to_column(row, 16, 81)[0:9]
    k_rows = jnp.concatenate([k1t[...], jnp.zeros((112, chan), F32)], axis=0)
    normed_taps = inv_l * (dot(gram, k_rows, precision=EXACT)[0:9] - single * mean_l)
    grad_taps = factor_l * (ten[0:9] - (bias_sum * single + gain_sum * normed_taps) / total)
    for i in range(3):
        kernel_one[i] = grad_taps[3 * i : 3 * i + 3]
    stores.append(pltpu.make_async_copy(kernel_one, kernel_one_hbm, sems.at[4]))
    stores[-1].start()
    for store in stores:
        store.wait()


def run(kernel, outs, scratch, *args, hbm=0, apart=(), flops=10**8, size=4 * 10**6):
    vmem = pl.BlockSpec(memory_space=pltpu.VMEM)
    devices = lax.axis_size("mel") * lax.axis_size("tm")
    specs = []
    args = list(args)
    for n, a in enumerate(args):
        if hbm and n >= len(args) - hbm:
            specs.append(pl.BlockSpec(memory_space=pltpu.HBM))
            args[n] = pltpu.with_memory_space_constraint(a, pltpu.HBM)
        else:
            specs.append(vmem)
            args[n] = pltpu.with_memory_space_constraint(a, pltpu.VMEM)
    return pl.pallas_call(
        kernel,
        out_shape=outs,
        in_specs=specs,
        out_specs=[pl.BlockSpec(memory_space=pltpu.HBM) if n in apart else vmem for n in range(len(outs))],
        scratch_shapes=scratch,
        compiler_params=pltpu.CompilerParams(vmem_limit_bytes=(29 + devices // 32) * 2**20),
        cost_estimate=pl.CostEstimate(flops=flops, bytes_accessed=size, transcendentals=0),
    )(*args)


def shape(dims, dtype=F32):
    return jax.ShapeDtypeStruct(dims, dtype)


def kept(dims, dtype=F32):
    return pltpu.VMEM(dims, dtype)


def far(dims, dtype=F32):
    return pltpu.HBM(dims, dtype)


def exchange(blocks, axes=AXES):
    return lax.all_to_all(blocks, axes, 0, 0, tiled=True)


def exchange_rows(rows, axes=AXES):
    return exchange(rows[:, None, :], axes)[:, 0, :]


def shards(spectrum, clip_bounds, kernel_one, gain_one, bias_one, kernel_two, gain_two, bias_two, pooled_grad):
    _, rows, frame_dev = spectrum.shape
    chan = kernel_two.shape[0]
    n_mel, n_tm = lax.axis_size("mel"), lax.axis_size("tm")
    devices = n_mel * n_tm
    half = frame_dev // 2
    wide = frame_dev + RIM
    mels = n_mel * rows

    packed, own, spec, masks = run(
        pack,
        [
            kept((devices, FIRST, 128), BF16),
            kept(pooled_grad.shape, BF16),
            kept(spectrum.shape, BF16),
            kept((8, wide)),
        ],
        [
            pltpu.SMEM(clip_bounds.shape, jnp.int32),
            pltpu.VMEM((2 * chan, half), F32),
            pltpu.VMEM((devices * FIRST, 128), F32),
            pltpu.SemaphoreType.DMA((3,)),
        ],
        spectrum,
        pooled_grad,
        clip_bounds,
        hbm=3,
    )
    recv = exchange(packed)
    ext = rows + 6
    span = 4 * 3 * chan
    wf, wb, w1, ws, pairs, singles, k1t, params, all_masks, edge_masks, twice, own_rows = run(
        weights,
        [
            kept((2 * chan, span), BF16),
            kept((2 * chan, span), BF16),
            kept((ext * chan, 128), BF16),
            far((rows * 8, (rows + 2) * chan), BF16),
            kept((chan, 128)),
            kept((chan, 128)),
            kept((16, chan)),
            kept((8, chan)),
            kept((3 * n_tm, frame_dev)),
            kept((n_tm * 8, 128)),
            kept((128, 128)),
            kept((chan * rows // 2, half), BF16),
        ],
        [
            pltpu.VMEM((9, chan, chan), BF16),
            pltpu.VMEM((3, 3, chan), BF16),
            pltpu.VMEM((4, 1, chan), F32),
            pltpu.SMEM(clip_bounds.shape, jnp.int32),
            pltpu.VMEM((rows * 8, (rows + 2) * chan), BF16),
            pltpu.VMEM((chan * rows // 2, half), F32),
            pltpu.SemaphoreType.DMA((8,)),
        ],
        own,
        clip_bounds,
        jnp.transpose(kernel_two, (2, 3, 0, 1)).reshape(9, chan, chan),
        jnp.transpose(kernel_one, (1, 2, 0)),
        gain_one[None],
        bias_one[None],
        gain_two[None],
        bias_two[None],
        hbm=7,
        apart=(3,),
    )
    pre_two, payload, act, x3, stats_one, features = run(
        forward_one,
        [
            kept(((rows + 4) * chan, wide)),
            kept((devices, SECOND, 128), BF16),
            kept((ext * 3 * chan, wide), BF16),
            kept((128, wide), BF16),
            kept((2 * chan + 16, 128)),
            kept((8, 128)),
        ],
        [
            pltpu.VMEM((ext * chan, wide), F32),
            pltpu.VMEM((devices * FIRST, 128), F32),
            pltpu.VMEM((n_tm * 8, 128), F32),
            pltpu.VMEM((mels + 8, RIM), F32),
            pltpu.VMEM((devices * SECOND, 128), F32),
        ],
        recv,
        spec,
        pairs,
        singles,
        twice,
        w1,
        wf,
        params,
        masks,
        all_masks,
        edge_masks,
    )
    recv = exchange(payload)
    grad, payload, row_pairs, stats_two = run(
        backward_scaled,
        [
            kept(((rows + 4) * chan, wide)),
            kept((devices * sum_rows(devices, 9 * chan), 128)),
            kept((rows // 2 * chan, frame_dev)),
            kept((chan + 8, 128)),
        ],
        [
            pltpu.VMEM(((rows // 2 + 2) * chan, RIM), F32),
            pltpu.VMEM(((rows // 2 + 2) * chan, frame_dev), F32),
            pltpu.VMEM((3 * chan + 16, rows * frame_dev), BF16),
            pltpu.VMEM((devices * SECOND, 128), F32),
            pltpu.VMEM((2 * chan, half), F32),
        ],
        recv,
        pre_two,
        act,
        own_rows,
        params,
        masks,
    )
    recv = exchange_rows(payload)
    low, payload, totals = run(
        backward,
        [
            kept(((rows + 2) * chan, wide), BF16),
            kept((devices * 14, 128)),
            kept((8, 128)),
        ],
        [
            pltpu.VMEM(((rows + 4) * 3 * chan, wide), BF16),
            pltpu.VMEM(((rows + 2) * chan, wide), F32),
            pltpu.VMEM((rows * chan, frame_dev), F32),
        ],
        recv,
        pre_two,
        grad,
        stats_two,
        w1,
        x3,
        stats_one,
        params,
        masks,
        wb,
    )
    recv = exchange_rows(payload)
    pooled, gain_two_grad, bias_two_grad = run(
        pool,
        [shape((1, chan, rows // 2, half), BF16), shape((1, chan)), shape((1, chan))],
        [
            pltpu.VMEM((rows // 2 * chan, 128), F32),
        ],
        totals,
        row_pairs,
    )
    first, normed, ws = run(
        transposed,
        [
            kept((rows * 8, wide)),
            kept(((rows + 2) * chan, wide), BF16),
            kept((rows * 8, (rows + 2) * chan), BF16),
        ],
        [pltpu.VMEM(((rows + 2) * chan, wide), F32), pltpu.SemaphoreType.DMA],
        low,
        w1,
        x3,
        stats_one,
        masks,
        ws,
        hbm=1,
    )
    spec_grad, kernel_one_grad, kernel_two_grad, gain_one_grad, bias_one_grad = run(
        finish,
        [
            shape((1, rows, frame_dev)),
            shape((3, 3, chan)),
            shape((9, chan, chan)),
            shape((1, chan)),
            shape((1, chan)),
        ],
        [
            pltpu.VMEM((3, rows * 8, 128), F32),
            pltpu.VMEM((1, rows, frame_dev), F32),
            pltpu.VMEM((3, 3, chan), F32),
            pltpu.VMEM((9, chan, chan), F32),
            pltpu.VMEM((1, chan), F32),
            pltpu.VMEM((1, chan), F32),
            pltpu.SemaphoreType.DMA((5,)),
        ],
        recv,
        features,
        stats_one,
        k1t,
        first,
        normed,
        ws,
        params,
        masks,
        apart=range(5),
    )
    kernel_two_grad = jnp.transpose(kernel_two_grad.reshape(3, 3, chan, chan), (2, 3, 0, 1))
    return (
        pooled,
        spec_grad,
        jnp.transpose(kernel_one_grad, (2, 0, 1)),
        gain_one_grad[0],
        bias_one_grad[0],
        kernel_two_grad,
        gain_two_grad[0],
        bias_two_grad[0],
    )


def solution(mesh):
    return jax.shard_map(
        shards,
        mesh=mesh,
        in_specs=(
            P(None, "mel", "tm"),
            P(),
            P(),
            P(),
            P(),
            P(),
            P(),
            P(),
            P(None, None, "mel", "tm"),
        ),
        out_specs=(P(None, None, "mel", "tm"), P(None, "mel", "tm"), P(), P(), P(), P(), P(), P()),
        check_vma=False,
    )
```

```python
import math

import jax
import jax.numpy as jnp
from jax import lax
from jax.experimental import pallas as pl
from jax.experimental.pallas import tpu as pltpu
from jax.sharding import PartitionSpec as P

F32 = jnp.float32
BF16 = jnp.bfloat16
AXES = ("mel", "tm")
EXACT = lax.Precision.HIGHEST
RIM = 128
BAND = 24
MEL_ROWS = 16
FIRST = 24
SUMS, EDGES, COLUMNS = 16, 19, 23
SIDE = 96
SECOND = 8


def iota(shape, dim):
    return lax.broadcasted_iota(jnp.int32, shape, dim)


def dot(a, b, over=((1,), (0,)), precision=None):
    return lax.dot_general(a, b, (over, ((), ())), precision=precision, preferred_element_type=F32)


def to_column(lanes, count, start=0):
    shape = (count, lanes.shape[1])
    return jnp.sum(jnp.where(iota(shape, 1) == iota(shape, 0) + start, lanes, 0.0), axis=1, keepdims=True)


def to_lanes(column, start=0, width=128):
    shape = (column.shape[0], width)
    return jnp.sum(jnp.where(iota(shape, 1) == iota(shape, 0) + start, column, 0.0), axis=0, keepdims=True)


def halves(v):
    total = v[:, :128]
    for n in range(128, v.shape[1], 128):
        total = total + v[:, n : n + 128]
    return total


def frame_masks(bounds, frames):
    last = bounds.shape[1] - 1

    def living(f):
        return (f >= 0) & (f < bounds[0, last])

    def paired(f):
        both = living(f) & living(f + 1)
        for k in range(1, last):
            both = both & (f + 1 != bounds[0, k])
        return both

    return tuple(m.astype(F32) for m in (living(frames), paired(frames - 1), paired(frames)))


def row_valid(row, rows):
    mel = lax.axis_index("mel") * rows + row
    return ((mel >= 0) & (mel < lax.axis_size("mel") * rows)).astype(F32)


def start_all(*pairs, sems):
    copies = [pltpu.make_async_copy(src, dst, sems.at[n]) for n, (src, dst) in enumerate(pairs)]
    for copy in copies:
        copy.start()
    return copies


def wait_all(copies):
    for copy in copies:
        copy.wait()


def joined_frames(parts, behind, ahead):
    third = parts.shape[0] // 3
    before, after = shifted_frames(parts[:third], behind, 1.0)[0], shifted_frames(parts[2 * third :], 1.0, ahead)[1]
    return parts[third : 2 * third] + before + after


def shifted_frames(value, behind, ahead):
    wide = value.shape[1]
    return pltpu.roll(value, 1, 1) * behind, pltpu.roll(value, wide - 1, 1) * ahead


def three_parts(v):
    high = lax.reduce_precision(v, 8, 7)
    mid = lax.reduce_precision(v - high, 8, 7)
    return high, mid, v - high - mid


def share_of(devices, chan):
    return -(-chan // devices)


def pack(spec_hbm, grad_hbm, bounds_hbm, out, own, spec, masks, bounds, edges, rows_out, sems):
    copies = start_all((bounds_hbm, bounds), (spec_hbm, spec), (grad_hbm, own), sems=sems)
    copies[0].wait()
    wide = masks.shape[1]
    frame_dev = wide - RIM
    devices = out.shape[0]
    rows = MEL_ROWS
    lane = iota((1, wide), 1)
    frames = lax.axis_index("tm") * frame_dev + jnp.where(lane < frame_dev + RIM // 2, lane, lane - wide)
    last = bounds.shape[1] - 1
    pixels = (bounds[0, last] * (lax.axis_size("mel") * rows)).astype(F32)
    found = frame_masks(bounds, frames)
    masks[...] = jnp.concatenate(
        list(found) + [jnp.full((1, wide), 1.0) * pixels, jnp.zeros((4, wide), F32)], axis=0
    )
    usable, behind, ahead = (m[:, :frame_dev] for m in found)
    copies[1].wait()
    x = spec[0].astype(F32) * usable
    lane = iota((1, frame_dev), 1)
    row = iota((rows, 1), 0)
    inner = jnp.where((lane > 0) & (lane < frame_dev - 1), usable, 0.0)
    number = (rows - 2) * jnp.sum(inner, axis=1, keepdims=True)
    inner = inner * ((row > 0) & (row < rows - 1)).astype(F32)
    centre = jnp.sum(jnp.sum(x, axis=0, keepdims=True), axis=1, keepdims=True)
    centre = centre / (rows * jnp.maximum(jnp.sum(usable, axis=1, keepdims=True), 1.0))
    centre = lax.reduce_precision(centre, 8, 7)
    shifted = [pltpu.roll(x, 1, 1) * behind, x, pltpu.roll(x, frame_dev - 1, 1) * ahead]
    taps = [pltpu.roll(v, (1 - i) % rows, 0) if i != 1 else v for i in range(3) for v in shifted]
    features = feature_rows(centre, (taps, inner))
    lane = iota((1, 128), 1)
    features = jnp.where(lane == 90, centre, jnp.where(lane == 91, number, features))
    pick = iota((8, frame_dev), 0)
    column = jnp.where(pick < 4, pick, frame_dev - 8 + pick)
    strip = dot((iota((8, frame_dev), 1) == column).astype(BF16), x.astype(BF16), ((1,), (1,)))
    lane = iota((8, 128), 1)
    repeat = (iota((rows, 128), 1) % rows == iota((rows, 128), 0)).astype(BF16)
    strip = jnp.where(lane // rows == iota((8, 128), 0), dot(strip.astype(BF16), repeat), 0.0)
    strip = jnp.sum(strip, axis=0, keepdims=True)

    def put(n, value):
        rows_out[pl.ds(n, devices, stride=FIRST), :] = jnp.broadcast_to(value, (devices, 128))

    near = jnp.concatenate([x[0:4], x[rows - 4 :]], axis=0)
    near = jnp.concatenate([near[:, :128], near[:, 128:]], axis=0)
    for d in range(devices):
        rows_out[FIRST * d : FIRST * d + 16, :] = near
    put(COLUMNS, strip)
    copies[2].wait()
    _, chan, many, half = own.shape
    share = share_of(devices, chan)
    holders = chan // share
    g = own[0].astype(F32)
    edges[0:chan] = g[:, 0, :]
    edges[chan:] = g[:, many - 1, :]

    def spread_out(v):
        if holders < devices:
            v = jnp.concatenate([v, jnp.zeros((devices - holders, 128), F32)], axis=0)
        return v

    for n in range(share):
        put(EDGES + n, spread_out(edges[n * holders : (n + 1) * holders, :]))
        put(EDGES + share + n, spread_out(edges[chan + n * holders : chan + (n + 1) * holders, :]))
    for n in range(2 * share, COLUMNS - EDGES):
        put(EDGES + n, jnp.zeros((1, 128), F32))
    end = iota((8, half), 0)
    at = iota((8, half), 1)
    ends = ((end == 0) & (at == 0)) | ((end == 1) & (at == half - 1))
    columns = dot(ends.astype(BF16), g.reshape(chan * many, half).astype(BF16), ((1,), (1,)))
    group = 128 // many
    source = iota((128, 128), 0)
    lane = iota((group, 128), 1)
    mine = lane // many == iota((group, 128), 0)
    parts = three_parts(features)
    for n in range(2):
        side = jnp.zeros((holders, 128), F32)
        for m in range(share):
            move = (iota((128, 128), 1) == SIDE + many * m + source % many).astype(BF16)
            first = m * holders * many // 128
            block = [columns[n : n + 1, 128 * q : 128 * (q + 1)] for q in range(first, first + holders * many // 128)]
            block = jnp.concatenate([jnp.where(mine, v, 0.0) for v in block], axis=0)
            side = side + dot(block.astype(BF16), move)
        put(SUMS + n, spread_out(side) + parts[n])
    put(SUMS + 2, parts[2])
    out[...] = rows_out[...].reshape(out.shape).astype(BF16)


def weights(own, bounds_hbm, k2_hbm, k1_hbm, gain_one_hbm, bias_one_hbm, gain_two_hbm, bias_two_hbm,
            wf, wb, w1, ws_hbm, pairs, singles, k1t, params, all_masks, edge_masks, twice, own_rows,
            k2, k1, vectors, bounds, ws, temp, sems):
    loads = start_all(
        (bounds_hbm, bounds),
        (k2_hbm, k2),
        (k1_hbm, k1),
        (gain_one_hbm, vectors.at[0]),
        (bias_one_hbm, vectors.at[1]),
        (gain_two_hbm, vectors.at[2]),
        (bias_two_hbm, vectors.at[3]),
        sems=sems,
    )
    _, many, count, half = own.shape
    temp[...] = own[0].astype(F32).reshape(many * count, half)
    for r in range(count):
        own_rows[r * many : (r + 1) * many] = temp[pl.ds(r, many, stride=count), :].astype(BF16)
    wait_all(loads)
    chan = k2.shape[1]
    taps = [k2[t].astype(F32) for t in range(9)]
    rest = jnp.zeros((chan, chan), F32)
    for j in range(3):
        forward = jnp.concatenate([taps[3 * i + j] for i in range(3)] + [rest], axis=1)
        backward = jnp.concatenate([taps[8 - 3 * i - j].T for i in range(3)] + [rest], axis=1)
        for r in range(2):
            at = slice((2 * j + r) * chan, (2 * j + r + 1) * chan)
            wf[at] = (pltpu.roll(forward, chan, 1) if r else forward).astype(BF16)
            wb[at] = (pltpu.roll(backward, chan, 1) if r else backward).astype(BF16)
    full = jnp.concatenate([k1[n].astype(F32) for n in range(3)] + [jnp.zeros((7, chan), F32)], axis=0)
    low = [
        jnp.concatenate([full[3 * (2 - a) + 2 - b : 3 * (2 - a) + 3 - b] for a in range(3)], axis=1)
        for b in range(3)
    ]
    base = jnp.concatenate(low + [jnp.zeros((5, 3 * chan), F32)], axis=0)
    base = jnp.concatenate([base, jnp.zeros((8, ws.shape[1] - 3 * chan), F32)], axis=1)
    for m in range(ws.shape[0] // 8):
        ws[8 * m : 8 * m + 8] = (pltpu.roll(base, chan * m, 1) if m else base).astype(BF16)
    store_ws = pltpu.make_async_copy(ws, ws_hbm, sems.at[7])
    store_ws.start()
    count, frame_dev = all_masks.shape[0] // 3, all_masks.shape[1]
    frames = iota((count, frame_dev), 0) * frame_dev + iota((count, frame_dev), 1)
    for n, mask in enumerate(frame_masks(bounds, frames)):
        all_masks[n * count : (n + 1) * count] = mask
    q = iota(edge_masks.shape, 0)
    lane = iota(edge_masks.shape, 1)
    k = q % 8
    frames = (q // 8) * frame_dev + jnp.where(k < 4, k, k + frame_dev - 8)
    living, behind, ahead = frame_masks(bounds, frames)
    living = jnp.where((k == 0) | (k == 7), living, 0.0)
    edge_masks[...] = jnp.where(lane == 0, living, jnp.where(lane == 1, behind, jnp.where(lane == 2, ahead, 0.0)))
    params[...] = jnp.concatenate(
        [vectors[n] for n in range(4)] + [jnp.zeros((4, chan), F32)], axis=0
    )
    tap = iota((16, 128), 0)
    lane = iota((16, 128), 1)
    i = (tap * 11) >> 5
    ninth = (lane * 57) >> 9
    to_band = (lane == BAND * (tap - 3 * i) + i) & (tap < 9)
    to_left = (ninth == tap) & (tap < 9)
    to_right = (lane - 9 * ninth == tap) & (lane < 81)
    to_single = (lane == 81 + tap) & (tap < 9)
    source = iota((128, 128), 0) - 81
    lane = iota((128, 128), 1)
    ninth = (lane * 57) >> 9
    inside = (source >= 0) & (source < 9) & (lane < 81)
    twice[...] = jnp.where(inside, (source == ninth).astype(F32) + (source == lane - 9 * ninth).astype(F32), 0.0)
    k1t[...] = full
    k = full.astype(BF16)
    lanes = [dot(k, select.astype(BF16), ((0,), (0,))) for select in (to_band, to_left, to_right, to_single)]
    pairs[...] = lanes[1] * lanes[2]
    singles[...] = lanes[3]
    for m in range(w1.shape[0] // chan):
        w1[m * chan : (m + 1) * chan] = (pltpu.roll(lanes[0], m, 1) if m else lanes[0]).astype(BF16)
    store_ws.wait()


def feature_rows(centre, *parts):
    def folded(v):
        return jnp.sum(halves(v), axis=0, keepdims=True)

    rows = [jnp.zeros((1, 128), F32)] * 96
    for taps, weight in parts:
        z = [tap - centre for tap in taps]
        for s in range(9):
            left = z[s] * weight
            rows[81 + s] = rows[81 + s] + folded(left)
            for t in range(s, 9):
                rows[9 * s + t] = rows[9 * t + s] = rows[9 * s + t] + folded(left * z[t])
    return to_lanes(jnp.sum(jnp.concatenate(rows, axis=0), axis=1, keepdims=True))


def summed_blocks(ref, devices):
    block = ref.shape[0] // devices
    period = 8 // math.gcd(block, 8)
    step = period * block
    total = ref[0:step, :]
    for at in range(step, ref.shape[0], step):
        total = total + ref[at : at + step, :]
    result = total[0:block]
    for n in range(1, period):
        result = result + total[n * block : (n + 1) * block]
    return result


def moved_rows(v, step):
    if step == 0:
        return v
    count = v.shape[0]
    if abs(step) >= count:
        return jnp.zeros_like(v)
    zero = jnp.zeros((abs(step), v.shape[1]), v.dtype)
    if step > 0:
        return jnp.concatenate([zero, v[: count - step]], axis=0)
    return jnp.concatenate([v[-step:], zero], axis=0)


def silu_halves(h):
    t = jnp.tanh(h)
    one = 1.0 + t
    return h * one, one * (1.0 + h * (1.0 - t))


def forward_one(recv, spec, pairs, singles, twice, w1, wf, params, masks, all_masks, edge_masks,
                pre_two, payload, moved_act, x3, stats, features_out, act, pre_one, got, strips, halo, rows_out):
    devices = recv.shape[0]
    n_mel, count = lax.axis_size("mel"), lax.axis_size("tm")
    rows = MEL_ROWS
    mels = n_mel * rows
    wide = masks.shape[1]
    frame_dev = wide - RIM
    chan = params.shape[1]
    me_m, me_t = lax.axis_index("mel"), lax.axis_index("tm")
    usable, behind, ahead = (masks[n : n + 1] for n in range(3))
    total = masks[3:4, 0:1]
    got[...] = recv[...].astype(F32).reshape(devices * FIRST, 128)

    def every(n):
        return got[pl.ds(n, devices, stride=FIRST), :]

    lane = iota((count, 128), 1)
    bands = [got[pl.ds(FIRST * k * count + COLUMNS, count, stride=FIRST), :] for k in range(n_mel)]
    for c in range(8):
        column = jnp.zeros((count, 128), F32)
        for k, band in enumerate(bands):
            part = jnp.where(lane // rows == c, band, 0.0)
            column = column + (pltpu.roll(part, rows * (k - c) % 128, 1) if k != c else part)
        strips[pl.ds(c, count, stride=8), :] = column
    at = pl.multiple_of(FIRST * (jnp.maximum(me_m - 1, 0) * count + me_t), 8)
    above = got[pl.ds(at, 16), :] * (me_m > 0).astype(F32)
    at = pl.multiple_of(FIRST * (jnp.minimum(me_m + 1, n_mel - 1) * count + me_t), 8)
    below = got[pl.ds(at, 16), :] * (me_m < n_mel - 1).astype(F32)
    above = jnp.concatenate([above[4:8], above[12:16]], axis=1)
    below = jnp.concatenate([below[0:4], below[8:12]], axis=1)
    own = spec[0].astype(F32) * usable[:, :frame_dev]
    at = pl.multiple_of(8 * jnp.minimum(me_t + 1, count - 1), 8)
    after = strips[pl.ds(at, 8), :][:, :mels] * (me_t + 1 < count).astype(F32)
    at = pl.multiple_of(8 * jnp.maximum(me_t - 1, 0), 8)
    before = strips[pl.ds(at, 8), :][:, :mels] * (me_t > 0).astype(F32)
    sides = jnp.concatenate([after[0:4], before[4:8], jnp.zeros((8, mels), F32)], axis=0).astype(BF16)
    side = iota((16, RIM), 0)
    place = iota((16, RIM), 1) == jnp.where(side < 4, side, jnp.where(side < 8, side + RIM - 8, -1))
    halo[0:8] = jnp.zeros((8, RIM), F32)
    halo[mels : mels + 8] = jnp.zeros((8, RIM), F32)
    halo[4 : mels + 4] = dot(sides, place.astype(BF16), ((0,), (0,)))
    rim = halo[pl.ds(pl.multiple_of(me_m * rows, 8), BAND), :]
    near = jnp.concatenate([jnp.concatenate([above, own, below], axis=0), rim], axis=1)
    x3[...] = jnp.concatenate(
        [
            pltpu.roll(near, 1, 1) * behind,
            near,
            pltpu.roll(near, wide - 1, 1) * ahead,
            jnp.broadcast_to(usable, (BAND, wide)),
            jnp.zeros((128 - 4 * BAND, wide), F32),
        ],
        axis=0,
    ).astype(BF16)
    pre_one[...] = dot(w1[...], x3[...])
    lane = iota((1, 128), 1)
    parts = jnp.where(lane < 92, every(SUMS) + every(SUMS + 1) + every(SUMS + 2), 0.0)
    centres, numbers = parts[:, 90:91], parts[:, 91:92]
    centre = jnp.sum(centres * numbers, axis=0, keepdims=True)
    centre = centre / jnp.maximum(jnp.sum(numbers, axis=0, keepdims=True), 1.0)
    delta = centres - centre
    features = jnp.sum(parts + delta * numbers * jnp.where(lane < 81, delta, 1.0), axis=0, keepdims=True)
    moved = jnp.sum(delta * parts, axis=0, keepdims=True)
    def edge_row(k, n):
        first = FIRST * k * count + n
        return jnp.concatenate(
            [got[pl.ds(first, count, stride=FIRST), :], got[pl.ds(first + 8, count, stride=FIRST), :]], axis=1
        )

    edge_rows = [[edge_row(k, n) for n in (0, 1, 6, 7)] for k in range(n_mel)]
    zero = jnp.zeros((count, frame_dev), F32)
    rows_of = [[], [], []]
    for k, (top, second, fore, bottom) in enumerate(edge_rows):
        for n, v in enumerate((edge_rows[k - 1][3] if k else zero, top, second)):
            rows_of[n].append(v)
        for n, v in enumerate((fore, bottom, edge_rows[k + 1][0] if k + 1 < n_mel else zero)):
            rows_of[n].append(v)
    f_usable, f_behind, f_ahead = (all_masks[n * count : (n + 1) * count, :] for n in range(3))
    lane = iota((count, frame_dev), 1)

    def frame_before(v):
        v = pltpu.roll(v, 1, 1)
        return jnp.where(lane == 0, pltpu.roll(v, 1, 0), v) * f_behind

    def frame_after(v):
        v = pltpu.roll(v, frame_dev - 1, 1)
        return jnp.where(lane == frame_dev - 1, pltpu.roll(v, count - 1, 0), v) * f_ahead

    taps = []
    for group in rows_of:
        for move in (frame_before, lambda v: v, frame_after):
            taps.append(jnp.concatenate([move(v) for v in group], axis=1))
    f_usable = jnp.concatenate([f_usable] * (2 * n_mel), axis=1)
    borders = (taps, f_usable)
    edge = strips[...]
    q_usable, q_behind, q_ahead = (edge_masks[:, n : n + 1] for n in range(3))
    lane = iota((count * 8, 128), 1)
    inside = (lane < mels) & (lane % rows != 0) & (lane % rows != rows - 1)
    shifted = [
        pltpu.roll(edge, 1, 0) * q_behind,
        edge,
        pltpu.roll(edge, count * 8 - 1, 0) * q_ahead,
    ]
    taps = [pltpu.roll(v, (1 - i) % 128, 1) if i != 1 else v for i in range(3) for v in shifted]
    features = features + feature_rows(centre, borders, (taps, jnp.where(inside, q_usable, 0.0)))
    features = jnp.where(iota((1, 128), 1) < 90, features, 0.0)
    near_mean = jnp.sum(singles[...] * features, axis=1, keepdims=True) / total
    around = jnp.sum(singles[...], axis=1, keepdims=True)
    square = jnp.sum(pairs[...] * features, axis=1, keepdims=True)
    square = (square + 2.0 * around * jnp.sum(singles[...] * moved, axis=1, keepdims=True)) / total
    inv = lax.rsqrt(square - near_mean * near_mean + 1e-05)
    mean = near_mean + centre * around
    lane = iota((chan, 128), 1)
    stats[0:chan] = jnp.where(lane == 0, mean, jnp.where(lane == 1, inv, 0.0))
    stats[chan : chan + 8] = jnp.broadcast_to(to_lanes(near_mean), (8, 128))
    stats[chan + 8 : chan + 16] = jnp.broadcast_to(to_lanes(inv), (8, 128))
    scale = 0.5 * to_column(params[0:1], chan) * inv
    shift = 0.5 * to_column(params[1:2], chan) - mean * scale
    stats[chan + 16 :] = jnp.where(lane == 0, scale, jnp.where(lane == 1, shift, 0.0))
    scale = jnp.broadcast_to(scale, (chan, wide))
    shift = jnp.broadcast_to(shift, (chan, wide))
    ext = w1.shape[0] // chan
    first = jnp.zeros((chan, 128), F32)
    second = jnp.zeros((chan, 128), F32)
    own_mask = usable[:, :frame_dev]
    low_masks = [m.astype(BF16) for m in (usable, behind, ahead)]
    for r in range(ext):
        value, _ = silu_halves(pre_one[r * chan : (r + 1) * chan, :] * scale + shift)
        if not 0 <= r - 3 < rows:
            value = value * row_valid(r - 3, rows)
        low = value.astype(BF16) * low_masks[0]
        act[r * chan : (r + 1) * chan, :] = low
        if 2 <= r < rows + 4:
            base = (r - 2) * 3 * chan
            for n, v in enumerate((low,) + shifted_frames(low, *low_masks[1:])):
                at = base + (1, 0, 2)[n] * chan
                moved_act[at : at + chan, :] = v[:, :frame_dev]
        if r < 3 or r % 2 == 0:
            continue
        g = (r - 3) // 2
        result = joined_frames(dot(wf[...], act[2 * g * chan : (2 * g + 4) * chan, :]), behind, ahead)
        pre_two[2 * g * chan : (2 * g + 2) * chan] = result
        for q in range(2):
            if 2 <= 2 * g + q < rows + 2:
                p = result[q * chan : (q + 1) * chan, :frame_dev]
                masked = p * own_mask
                first = first + halves(masked)
                second = second + halves(masked * p)
    moved = dot(jnp.broadcast_to(moved, (8, 128)), twice[...], precision=EXACT)[0:1]
    features_out[...] = jnp.concatenate(
        [features + moved, jnp.broadcast_to(centre, (1, 128)), jnp.zeros((6, 128), F32)], axis=0
    )
    share = share_of(devices, chan)

    def put(n, value):
        rows_out[pl.ds(n, devices, stride=SECOND), :] = jnp.broadcast_to(value, (devices, 128))

    for n in range(share):
        put(3 + n, moved_rows(every(EDGES + share + n), count))
        put(3 + share + n, moved_rows(every(EDGES + n), -count))
    for n in range(3 + 2 * share, SECOND - 1):
        put(n, jnp.zeros((1, 128), F32))
    lane = iota((devices, 128), 1)
    tm = iota((devices, 128), 0) % count
    lefts = jnp.where(lane >= SIDE, every(SUMS), 0.0)
    rights = jnp.where(lane >= SIDE, every(SUMS + 1), 0.0)
    beside = jnp.zeros((devices, 128), F32)
    for n, step in enumerate((0, count, -count)):
        one = jnp.where(tm > 0, moved_rows(rights, step + 1), 0.0)
        two = jnp.where(tm < count - 1, moved_rows(lefts, step - 1), 0.0)
        beside = beside + pltpu.roll(one, (32 * n - SIDE) % 128, 1) + pltpu.roll(two, (32 * n + 16 - SIDE) % 128, 1)
    put(SECOND - 1, beside)
    first = jnp.sum(first, axis=1, keepdims=True)
    second = jnp.sum(second, axis=1, keepdims=True)
    for n, part in enumerate(three_parts(to_lanes(first) + to_lanes(second, chan))):
        put(n, part)
    payload[...] = rows_out[...].reshape(payload.shape).astype(BF16)


def sum_rows(devices, taps):
    return -(-taps // devices) + 2


def backward_scaled(recv, pre_two, act, own_rows, params, masks,
                    grad, payload, pairs, stats, sides, up, right, got, beyond):
    devices = recv.shape[0]
    got[...] = recv[...].astype(F32).reshape(devices * SECOND, 128)
    chan = params.shape[1]
    half = own_rows.shape[1]
    lane = iota((half, 2 * half), 1)
    spread = jnp.where(lane >> 1 == iota((half, 2 * half), 0), 0.25, 0.0).astype(BF16)
    rows = MEL_ROWS
    wide = pre_two.shape[1]
    frame_dev = wide - RIM
    usable = masks[0:1]
    share = share_of(devices, chan)
    holders = chan // share

    def every(n):
        return got[pl.ds(n, devices, stride=SECOND), :]

    beside = every(SECOND - 1)[:holders]
    lane = iota((holders, RIM), 1)
    many = rows // 2
    up[0 : many * chan] = dot(own_rows[...], spread)
    for n in range(share):
        first = n * holders
        beyond[first : first + holders, :] = every(3 + n)[:holders]
        beyond[chan + first : chan + first + holders, :] = every(3 + share + n)[:holders]
        for r in range(many + 2):
            at = many * n + (r if r < many else 32 + many - 1 if r == many else 64)
            left, right_of = beside[:, at : at + 1], beside[:, at + 16 : at + 17]
            side = jnp.where(lane >= RIM - 2, 0.25 * left, jnp.where(lane < 2, 0.25 * right_of, 0.0))
            sides[r * chan + first : r * chan + first + holders, :] = side
    up[many * chan :] = dot(beyond[...].astype(BF16), spread)
    total = masks[3:4, 0:1]
    sums = jnp.sum(every(0) + every(1) + every(2), axis=0, keepdims=True)
    mean = to_column(sums, chan) / total
    inv = lax.rsqrt(to_column(sums, chan, chan) / total - mean * mean + 1e-05)
    lane = iota((chan, 128), 1)
    scale = 0.5 * to_column(params[2:3], chan) * inv
    shift = 0.5 * to_column(params[3:4], chan) - mean * scale
    columns = jnp.zeros((chan, 128), F32)
    for n, column in enumerate((mean, inv, scale, shift)):
        columns = jnp.where(lane == n, column, columns)
    stats[0:chan] = columns
    stats[chan : chan + 8] = jnp.broadcast_to(to_lanes(inv), (8, 128))
    shift = jnp.broadcast_to(shift, (chan, wide))
    scale = jnp.broadcast_to(scale, (chan, wide))
    mean = jnp.broadcast_to(mean, (chan, frame_dev))
    inv = jnp.broadcast_to(inv, (chan, frame_dev))
    first = jnp.zeros((chan, 128), F32)
    second = jnp.zeros((chan, 128), F32)
    own_mask = usable[:, :frame_dev]
    right[3 * chan :] = jnp.ones((16, rows * frame_dev), BF16)
    table = jnp.zeros((9 * chan, 3 * chan + 16), F32)
    for q in list(range(2, rows + 2)) + [0, 1, rows + 2, rows + 3]:
        r = q // 2
        at = slice(q * chan, (q + 1) * chan)
        m = q - 2
        mask = 0.5 * usable if 0 <= m < rows else usable * (0.5 * row_valid(m, rows))
        if q % 2 == 0:
            spot = (r - 1 if 1 <= r <= many else many + (r > 0)) * chan
            upstream = jnp.concatenate([up[spot : spot + chan, :], sides[spot : spot + chan, :]], axis=1)
        pre = pre_two[at, :]
        value, slope = silu_halves(pre * scale + shift)
        g = upstream * slope * mask
        grad[at, :] = g
        if not 0 <= m < rows:
            continue
        g = g[:, :frame_dev]
        normed = (pre[:, :frame_dev] - mean) * inv
        first = first + halves(g * normed)
        second = second + halves(g)
        value = value[:, :frame_dev] * own_mask
        both = value if m % 2 == 0 else both + value
        if m % 2:
            pairs[(r - 1) * chan : r * chan, :] = both
        lanes = slice(m * frame_dev, (m + 1) * frame_dev)
        right[0:chan, lanes] = g.astype(BF16)
        right[chan : 2 * chan, lanes] = normed.astype(BF16)
        right[2 * chan : 3 * chan, lanes] = (g - right[0:chan, lanes].astype(F32)).astype(BF16)
        if m in (5, 11, rows - 1):
            start = m - m % 6
            left = [act[n * 3 * chan : (n + 3) * 3 * chan, :] for n in range(start, m + 1)]
            lanes = slice(start * frame_dev, (m + 1) * frame_dev)
            table = table + dot(jnp.concatenate(left, axis=1), right[:, lanes], ((1,), (1,)))
    first = jnp.sum(first, axis=1, keepdims=True)
    second = jnp.sum(second, axis=1, keepdims=True)
    totals = to_lanes(first) + to_lanes(second, chan)
    block = payload.shape[0] // devices
    payload[pl.ds(0, devices, stride=block), :] = jnp.broadcast_to(totals, (devices, 128))
    rest = jnp.concatenate([table[:, 2 * chan :], jnp.zeros((9 * chan, chan - 16), F32)], axis=1)
    both = table[:, : 2 * chan] + jnp.where(iota(rest.shape, 1) < chan, rest, 0.0)
    single = rest[:, chan : chan + 1]
    lane = iota((devices, 128), 1)
    constants = jnp.zeros((devices, 128), F32)
    for k in range(block - 2):
        cut, ones = both[k * devices : (k + 1) * devices], single[k * devices : (k + 1) * devices]
        short = devices - cut.shape[0]
        if short:
            cut = jnp.concatenate([cut, jnp.zeros((short, 128), F32)], axis=0)
            ones = jnp.concatenate([ones, jnp.zeros((short, 1), F32)], axis=0)
        payload[pl.ds(1 + k, devices, stride=block), :] = cut
        constants = jnp.where(lane == k, ones, constants)
    payload[pl.ds(block - 1, devices, stride=block), :] = constants


def pool(totals, pairs, out, gain_out, bias_out, temp):
    gain_out[...] = totals[0:1, : gain_out.shape[1]]
    bias_out[...] = totals[0:1, gain_out.shape[1] :]
    chan, rows, half = out.shape[1:]
    to_mean = jnp.where(iota((2 * half, half), 0) >> 1 == iota((2 * half, half), 1), 0.25, 0.0)
    pooled = dot(pairs[...], to_mean, precision=EXACT)
    for r in range(rows):
        temp[pl.ds(r, chan, stride=rows), :] = pooled[r * chan : (r + 1) * chan]
    out[0] = temp[...].reshape(chan, rows, half).astype(BF16)


def backward(recv, pre_two, grad, stats_two, w1, x3, stats, params, masks, wb,
             out, payload, totals, grad_low, pre_one, g1):
    chan = params.shape[1]
    rows = MEL_ROWS
    wide = pre_two.shape[1]
    frame_dev = wide - RIM
    usable, behind, ahead = (masks[n : n + 1] for n in range(3))
    total = masks[3:4, 0:1]
    devices = payload.shape[0] // 14
    pre_one[...] = dot(w1[2 * chan : (rows + 4) * chan], x3[...])

    received = summed_blocks(recv, devices)
    sums = received[0:1]
    gain_sum, bias_sum = sums[:, :chan], sums[:, chan:]
    totals[...] = jnp.broadcast_to(sums, (8, 128))
    mean, inv = stats_two[0:chan, 0:1], stats_two[0:chan, 1:2]
    factor = to_column(params[2:3], chan) * inv
    gain_part = factor * (to_column(sums, chan) / total * inv)
    bias_part = factor * (to_column(sums, chan, chan) / total) - mean * gain_part
    gain_part = jnp.broadcast_to(gain_part, (chan, wide))
    bias_part = jnp.broadcast_to(bias_part, (chan, wide))
    factor = jnp.broadcast_to(factor, (chan, wide))
    scale = jnp.broadcast_to(stats[chan + 16 :, 0:1], (chan, wide))
    shift = jnp.broadcast_to(stats[chan + 16 :, 1:2], (chan, wide))
    factor_one = jnp.broadcast_to(to_column(params[0:1], chan) * stats[0:chan, 1:2], (chan, wide))
    count = pre_two.shape[0] // chan
    table = jnp.zeros((chan, 128), F32)

    def tap_sums(m):
        part = g1[m * chan : (m + 4) * chan, :]
        high = lax.reduce_precision(part, 8, 7)
        low = (part - high).astype(BF16)
        taps_in = x3[:, :frame_dev]
        products = dot(high.astype(BF16), taps_in, ((1,), (1,))) + dot(low, taps_in, ((1,), (1,)))
        moved = [pltpu.roll(products[k * chan : (k + 1) * chan], 128 - (m + k + 3), 1) for k in range(4)]
        return (moved[0] + moved[1]) + (moved[2] + moved[3])

    for q in range(count):
        at = slice(q * chan, (q + 1) * chan)
        mask = usable if 0 <= q - 2 < rows else usable * row_valid(q - 2, rows)
        low = (factor * grad[at, :] - (bias_part + pre_two[at, :] * gain_part) * mask).astype(BF16)
        grad_low[q * chan : (q + 1) * chan, :] = low
        if q < 3 or q % 2 == 0:
            continue
        start = q - 3
        result = joined_frames(dot(wb[...], grad_low[start * chan : (start + 4) * chan, :]), behind, ahead)
        for n in range(2):
            m = start + n - 1
            at = slice((m + 1) * chan, (m + 2) * chan)
            _, slope = silu_halves(pre_one[at, :] * scale + shift)
            mask = 0.5 * usable if 0 <= m < rows else usable * (0.5 * row_valid(m, rows))
            value = result[n * chan : (n + 1) * chan] * slope * mask
            out[at, :] = (value * factor_one).astype(BF16)
            if not 0 <= m < rows:
                continue
            g1[m * chan : (m + 1) * chan, :] = value[:, :frame_dev]
            if m % 4 == 3 and m > 3:
                table = table + tap_sums(m - 7)
    table = table + tap_sums(rows - 4)
    tap = iota((16, 128), 0)
    lane = iota((16, 128), 1)
    i = (tap * 11) >> 5
    select = ((lane == BAND * (tap - 3 * i) + i) & (tap < 9)) | ((lane == 3 * BAND) & (tap == 9))
    rows10 = dot(select.astype(F32), table, ((1,), (1,)), EXACT)
    share = received.shape[0] - 2
    mine = received[1 : share + 1]
    single = to_column(received[share + 1 :], share)
    factor_l = params[2:3] * stats_two[chan : chan + 1, :chan]
    mine = mine[:, :chan] - (bias_sum * single + gain_sum * mine[:, chan:]) / total
    mine = factor_l * mine
    lower = -(-share // 2)
    mine = jnp.concatenate([mine] + [jnp.zeros((2 * lower - share, chan), F32)] * (share % 2), axis=0)
    mine = jnp.concatenate([mine[:lower], mine[lower:]], axis=1)
    if lower < 9:
        mine = jnp.concatenate([mine, jnp.zeros((9 - lower, 128), F32)], axis=0)
    sums = jnp.concatenate([rows10[0:5], rows10[5:10]], axis=1)
    block = jnp.concatenate([sums, mine], axis=0)
    block = jnp.concatenate([block] * 4, axis=0)
    for d in range(0, devices, 4):
        payload[14 * d : 14 * (d + 4), :] = block


def transposed(low, w1, x3, stats, masks, ws_hbm, first, normed, ws, pre_one, sem):
    load = pltpu.make_async_copy(ws_hbm, ws, sem)
    load.start()
    chan = low.shape[0] // (MEL_ROWS + 2)
    wide = low.shape[1]
    pre_one[...] = dot(w1[2 * chan : (MEL_ROWS + 4) * chan], x3[...])
    mean = jnp.broadcast_to(stats[0:chan, 0:1], (chan, wide))
    inv = jnp.broadcast_to(stats[0:chan, 1:2], (chan, wide))
    for q in range(MEL_ROWS + 2):
        at = slice(q * chan, (q + 1) * chan)
        mask = masks[0:1] * row_valid(q - 1, MEL_ROWS)
        normed[at, :] = ((pre_one[at, :] - mean) * inv * mask).astype(BF16)
    load.wait()
    first[...] = dot(ws[...], low[...])


def finish(recv, features, stats, k1t, first, normed, ws, params, masks,
           spec_hbm, kernel_one_hbm, kernel_two_hbm, gain_hbm, bias_hbm,
           table, spec_grad, kernel_one, kernel_two, gain_out, bias_out, sems):
    chan = params.shape[1]
    rows = MEL_ROWS
    wide = normed.shape[1]
    frame_dev = wide - RIM
    usable, behind, ahead = (masks[n : n + 1] for n in range(3))
    total = masks[3:4, 0:1]
    gain = params[0:1]
    count = recv.shape[0] // 14
    share = -(-9 * chan // count)
    lower = -(-share // 2)
    left = [recv[pl.ds(5 + p, count, stride=14), :] for p in range(lower)]
    whole = jnp.concatenate([v[:, :chan] for v in left] + [v[:, chan:] for v in left], axis=0)
    for t in range(9):
        kernel_two[t] = whole[t * chan : (t + 1) * chan].T
    stores = [pltpu.make_async_copy(kernel_two, kernel_two_hbm, sems.at[3])]
    stores[0].start()
    sums = summed_blocks(recv, count)[0:5]
    ten = jnp.concatenate([sums[:, :chan], sums[:, chan:]], axis=0)
    bias_sum = ten[9:10]
    mean_l, inv_l = stats[chan : chan + 1, :chan], stats[chan + 8 : chan + 9, :chan]
    ten = ten - features[1:2, 0:1] * bias_sum
    k = k1t[0:9]
    gain_sum = inv_l * (jnp.sum(k * ten[0:9], axis=0, keepdims=True) - mean_l * bias_sum)
    gain_out[...] = gain_sum
    bias_out[...] = bias_sum
    for n, (source, target) in enumerate(((gain_out, gain_hbm), (bias_out, bias_hbm))):
        stores.append(pltpu.make_async_copy(source, target, sems.at[n]))
        stores[-1].start()
    factor_l = gain * inv_l
    scale = factor_l * gain_sum / total
    scale = jnp.concatenate([scale, scale], axis=1)
    scale = jnp.concatenate([scale] * ((rows + 2) // 2), axis=1)
    taps = first[...] - dot((ws[...].astype(F32) * scale).astype(BF16), normed[...])
    for part in range(wide // 128):
        table[part] = taps[:, 128 * part : 128 * (part + 1)]
    moved = [
        jnp.concatenate([table[part, pl.ds(b, rows, stride=8), :] for part in range(wide // 128)], axis=1)
        for b in range(3)
    ]
    constant = jnp.sum(k * (factor_l * bias_sum / total), axis=1, keepdims=True)
    for a in range(3):
        row = iota((rows, 1), 0) + (a - 1) + lax.axis_index("mel") * rows
        valid = ((row >= 0) & (row < lax.axis_size("mel") * rows)).astype(F32) * usable
        for b in range(3):
            t = 3 * (2 - a) + 2 - b
            moved[b] = moved[b] - constant[t : t + 1] * valid
    result = pltpu.roll(moved[0], 1, 1) * behind + moved[1] + pltpu.roll(moved[2], wide - 1, 1) * ahead
    spec_grad[0] = (result * usable)[:, :frame_dev]
    stores.append(pltpu.make_async_copy(spec_grad, spec_hbm, sems.at[2]))
    stores[-1].start()
    row = features[0:1, :]
    lane = iota((1, 128), 1)
    gram = jnp.concatenate(
        [jnp.where(lane < 9, pltpu.roll(row, 128 - 9 * t, 1) if t else row, 0.0) for t in range(9)]
        + [jnp.zeros((7, 128), F32)],
        axis=0,
    )
    single = to_column(row, 16, 81)[0:9]
    k_rows = jnp.concatenate([k1t[...], jnp.zeros((112, chan), F32)], axis=0)
    normed_taps = inv_l * (dot(gram, k_rows, precision=EXACT)[0:9] - single * mean_l)
    grad_taps = factor_l * (ten[0:9] - (bias_sum * single + gain_sum * normed_taps) / total)
    for i in range(3):
        kernel_one[i] = grad_taps[3 * i : 3 * i + 3]
    stores.append(pltpu.make_async_copy(kernel_one, kernel_one_hbm, sems.at[4]))
    stores[-1].start()
    for store in stores:
        store.wait()


def run(kernel, outs, scratch, *args, hbm=0, apart=(), flops=10**8, size=4 * 10**6):
    vmem = pl.BlockSpec(memory_space=pltpu.VMEM)
    devices = lax.axis_size("mel") * lax.axis_size("tm")
    specs = []
    args = list(args)
    for n, a in enumerate(args):
        if hbm and n >= len(args) - hbm:
            specs.append(pl.BlockSpec(memory_space=pltpu.HBM))
            args[n] = pltpu.with_memory_space_constraint(a, pltpu.HBM)
        else:
            specs.append(vmem)
            args[n] = pltpu.with_memory_space_constraint(a, pltpu.VMEM)
    return pl.pallas_call(
        kernel,
        out_shape=outs,
        in_specs=specs,
        out_specs=[pl.BlockSpec(memory_space=pltpu.HBM) if n in apart else vmem for n in range(len(outs))],
        scratch_shapes=scratch,
        compiler_params=pltpu.CompilerParams(vmem_limit_bytes=(29 + devices // 32) * 2**20),
        cost_estimate=pl.CostEstimate(flops=flops, bytes_accessed=size, transcendentals=0),
    )(*args)


def shape(dims, dtype=F32):
    return jax.ShapeDtypeStruct(dims, dtype)


def kept(dims, dtype=F32):
    return pltpu.VMEM(dims, dtype)


def far(dims, dtype=F32):
    return pltpu.HBM(dims, dtype)


def exchange(blocks, axes=AXES):
    return lax.all_to_all(blocks, axes, 0, 0, tiled=True)


def exchange_rows(rows, axes=AXES):
    return exchange(rows[:, None, :], axes)[:, 0, :]


def shards(spectrum, clip_bounds, kernel_one, gain_one, bias_one, kernel_two, gain_two, bias_two, pooled_grad):
    _, rows, frame_dev = spectrum.shape
    chan = kernel_two.shape[0]
    n_mel, n_tm = lax.axis_size("mel"), lax.axis_size("tm")
    devices = n_mel * n_tm
    half = frame_dev // 2
    wide = frame_dev + RIM
    mels = n_mel * rows

    packed, own, spec, masks = run(
        pack,
        [
            kept((devices, FIRST, 128), BF16),
            kept(pooled_grad.shape, BF16),
            kept(spectrum.shape, BF16),
            kept((8, wide)),
        ],
        [
            pltpu.SMEM(clip_bounds.shape, jnp.int32),
            pltpu.VMEM((2 * chan, half), F32),
            pltpu.VMEM((devices * FIRST, 128), F32),
            pltpu.SemaphoreType.DMA((3,)),
        ],
        spectrum,
        pooled_grad,
        clip_bounds,
        hbm=3,
    )
    recv = exchange(packed)
    ext = rows + 6
    wf, wb, w1, ws, pairs, singles, k1t, params, all_masks, edge_masks, twice, own_rows = run(
        weights,
        [
            kept((6 * chan, 4 * chan), BF16),
            kept((6 * chan, 4 * chan), BF16),
            kept((ext * chan, 128), BF16),
            far((rows * 8, (rows + 2) * chan), BF16),
            kept((chan, 128)),
            kept((chan, 128)),
            kept((16, chan)),
            kept((8, chan)),
            kept((3 * n_tm, frame_dev)),
            kept((n_tm * 8, 128)),
            kept((128, 128)),
            kept((chan * rows // 2, half), BF16),
        ],
        [
            pltpu.VMEM((9, chan, chan), BF16),
            pltpu.VMEM((3, 3, chan), BF16),
            pltpu.VMEM((4, 1, chan), F32),
            pltpu.SMEM(clip_bounds.shape, jnp.int32),
            pltpu.VMEM((rows * 8, (rows + 2) * chan), BF16),
            pltpu.VMEM((chan * rows // 2, half), F32),
            pltpu.SemaphoreType.DMA((8,)),
        ],
        own,
        clip_bounds,
        jnp.transpose(kernel_two, (2, 3, 0, 1)).reshape(9, chan, chan),
        jnp.transpose(kernel_one, (1, 2, 0)),
        gain_one[None],
        bias_one[None],
        gain_two[None],
        bias_two[None],
        hbm=7,
        apart=(3,),
    )
    pre_two, payload, act, x3, stats_one, features = run(
        forward_one,
        [
            kept(((rows + 4) * chan, wide)),
            kept((devices, SECOND, 128), BF16),
            kept(((rows + 2) * 3 * chan, frame_dev), BF16),
            kept((128, wide), BF16),
            kept((2 * chan + 16, 128)),
            kept((8, 128)),
        ],
        [
            pltpu.VMEM((ext * chan, wide), BF16),
            pltpu.VMEM((ext * chan, wide), F32),
            pltpu.VMEM((devices * FIRST, 128), F32),
            pltpu.VMEM((n_tm * 8, 128), F32),
            pltpu.VMEM((mels + 8, RIM), F32),
            pltpu.VMEM((devices * SECOND, 128), F32),
        ],
        recv,
        spec,
        pairs,
        singles,
        twice,
        w1,
        wf,
        params,
        masks,
        all_masks,
        edge_masks,
    )
    recv = exchange(payload)
    grad, payload, row_pairs, stats_two = run(
        backward_scaled,
        [
            kept(((rows + 4) * chan, wide)),
            kept((devices * sum_rows(devices, 9 * chan), 128)),
            kept((rows // 2 * chan, frame_dev)),
            kept((chan + 8, 128)),
        ],
        [
            pltpu.VMEM(((rows // 2 + 2) * chan, RIM), F32),
            pltpu.VMEM(((rows // 2 + 2) * chan, frame_dev), F32),
            pltpu.VMEM((3 * chan + 16, rows * frame_dev), BF16),
            pltpu.VMEM((devices * SECOND, 128), F32),
            pltpu.VMEM((2 * chan, half), F32),
        ],
        recv,
        pre_two,
        act,
        own_rows,
        params,
        masks,
    )
    recv = exchange_rows(payload)
    low, payload, totals = run(
        backward,
        [
            kept(((rows + 2) * chan, wide), BF16),
            kept((devices * 14, 128)),
            kept((8, 128)),
        ],
        [
            pltpu.VMEM(((rows + 4) * chan, wide), BF16),
            pltpu.VMEM(((rows + 2) * chan, wide), F32),
            pltpu.VMEM((rows * chan, frame_dev), F32),
        ],
        recv,
        pre_two,
        grad,
        stats_two,
        w1,
        x3,
        stats_one,
        params,
        masks,
        wb,
    )
    recv = exchange_rows(payload)
    pooled, gain_two_grad, bias_two_grad = run(
        pool,
        [shape((1, chan, rows // 2, half), BF16), shape((1, chan)), shape((1, chan))],
        [
            pltpu.VMEM((rows // 2 * chan, 128), F32),
        ],
        totals,
        row_pairs,
    )
    first, normed, ws = run(
        transposed,
        [
            kept((rows * 8, wide)),
            kept(((rows + 2) * chan, wide), BF16),
            kept((rows * 8, (rows + 2) * chan), BF16),
        ],
        [pltpu.VMEM(((rows + 2) * chan, wide), F32), pltpu.SemaphoreType.DMA],
        low,
        w1,
        x3,
        stats_one,
        masks,
        ws,
        hbm=1,
    )
    spec_grad, kernel_one_grad, kernel_two_grad, gain_one_grad, bias_one_grad = run(
        finish,
        [
            shape((1, rows, frame_dev)),
            shape((3, 3, chan)),
            shape((9, chan, chan)),
            shape((1, chan)),
            shape((1, chan)),
        ],
        [
            pltpu.VMEM((3, rows * 8, 128), F32),
            pltpu.VMEM((1, rows, frame_dev), F32),
            pltpu.VMEM((3, 3, chan), F32),
            pltpu.VMEM((9, chan, chan), F32),
            pltpu.VMEM((1, chan), F32),
            pltpu.VMEM((1, chan), F32),
            pltpu.SemaphoreType.DMA((5,)),
        ],
        recv,
        features,
        stats_one,
        k1t,
        first,
        normed,
        ws,
        params,
        masks,
        apart=range(5),
    )
    kernel_two_grad = jnp.transpose(kernel_two_grad.reshape(3, 3, chan, chan), (2, 3, 0, 1))
    return (
        pooled,
        spec_grad,
        jnp.transpose(kernel_one_grad, (2, 0, 1)),
        gain_one_grad[0],
        bias_one_grad[0],
        kernel_two_grad,
        gain_two_grad[0],
        bias_two_grad[0],
    )


def solution(mesh):
    return jax.shard_map(
        shards,
        mesh=mesh,
        in_specs=(
            P(None, "mel", "tm"),
            P(),
            P(),
            P(),
            P(),
            P(),
            P(),
            P(),
            P(None, None, "mel", "tm"),
        ),
        out_specs=(P(None, None, "mel", "tm"), P(None, "mel", "tm"), P(), P(), P(), P(), P(), P()),
        check_vma=False,
    )
```

```python
import math

import jax
import jax.numpy as jnp
from jax import lax
from jax.experimental import pallas as pl
from jax.experimental.pallas import tpu as pltpu
from jax.sharding import PartitionSpec as P

F32 = jnp.float32
BF16 = jnp.bfloat16
AXES = ("mel", "tm")
EXACT = lax.Precision.HIGHEST
RIM = 128
BAND = 24
MEL_ROWS = 16
FIRST = 24
SUMS, EDGES, COLUMNS = 16, 19, 23
SIDE = 96
SECOND = 8


def iota(shape, dim):
    return lax.broadcasted_iota(jnp.int32, shape, dim)


def dot(a, b, over=((1,), (0,)), precision=None):
    return lax.dot_general(a, b, (over, ((), ())), precision=precision, preferred_element_type=F32)


def to_column(lanes, count, start=0):
    shape = (count, lanes.shape[1])
    return jnp.sum(jnp.where(iota(shape, 1) == iota(shape, 0) + start, lanes, 0.0), axis=1, keepdims=True)


def to_lanes(column, start=0, width=128):
    shape = (column.shape[0], width)
    return jnp.sum(jnp.where(iota(shape, 1) == iota(shape, 0) + start, column, 0.0), axis=0, keepdims=True)


def halves(v):
    total = v[:, :128]
    for n in range(128, v.shape[1], 128):
        total = total + v[:, n : n + 128]
    return total


def frame_masks(bounds, frames):
    last = bounds.shape[1] - 1

    def living(f):
        return (f >= 0) & (f < bounds[0, last])

    def paired(f):
        both = living(f) & living(f + 1)
        for k in range(1, last):
            both = both & (f + 1 != bounds[0, k])
        return both

    return tuple(m.astype(F32) for m in (living(frames), paired(frames - 1), paired(frames)))


def row_valid(row, rows):
    mel = lax.axis_index("mel") * rows + row
    return ((mel >= 0) & (mel < lax.axis_size("mel") * rows)).astype(F32)


def start_all(*pairs, sems):
    copies = [pltpu.make_async_copy(src, dst, sems.at[n]) for n, (src, dst) in enumerate(pairs)]
    for copy in copies:
        copy.start()
    return copies


def wait_all(copies):
    for copy in copies:
        copy.wait()


def shifted_frames(value, behind, ahead):
    wide = value.shape[1]
    return pltpu.roll(value, 1, 1) * behind, pltpu.roll(value, wide - 1, 1) * ahead


def three_parts(v):
    high = lax.reduce_precision(v, 8, 7)
    mid = lax.reduce_precision(v - high, 8, 7)
    return high, mid, v - high - mid


def share_of(devices, chan):
    return -(-chan // devices)


def pack(spec_hbm, grad_hbm, bounds_hbm, out, own, spec, masks, bounds, edges, rows_out, sems):
    copies = start_all((bounds_hbm, bounds), (spec_hbm, spec), (grad_hbm, own), sems=sems)
    copies[0].wait()
    wide = masks.shape[1]
    frame_dev = wide - RIM
    devices = out.shape[0]
    rows = MEL_ROWS
    lane = iota((1, wide), 1)
    frames = lax.axis_index("tm") * frame_dev + jnp.where(lane < frame_dev + RIM // 2, lane, lane - wide)
    last = bounds.shape[1] - 1
    pixels = (bounds[0, last] * (lax.axis_size("mel") * rows)).astype(F32)
    found = frame_masks(bounds, frames)
    masks[...] = jnp.concatenate(
        list(found) + [jnp.full((1, wide), 1.0) * pixels, jnp.zeros((4, wide), F32)], axis=0
    )
    usable, behind, ahead = (m[:, :frame_dev] for m in found)
    copies[1].wait()
    x = spec[0].astype(F32) * usable
    lane = iota((1, frame_dev), 1)
    row = iota((rows, 1), 0)
    inner = jnp.where((lane > 0) & (lane < frame_dev - 1), usable, 0.0)
    number = (rows - 2) * jnp.sum(inner, axis=1, keepdims=True)
    inner = inner * ((row > 0) & (row < rows - 1)).astype(F32)
    centre = jnp.sum(jnp.sum(x, axis=0, keepdims=True), axis=1, keepdims=True)
    centre = centre / (rows * jnp.maximum(jnp.sum(usable, axis=1, keepdims=True), 1.0))
    centre = lax.reduce_precision(centre, 8, 7)
    shifted = [pltpu.roll(x, 1, 1) * behind, x, pltpu.roll(x, frame_dev - 1, 1) * ahead]
    taps = [pltpu.roll(v, (1 - i) % rows, 0) if i != 1 else v for i in range(3) for v in shifted]
    features = feature_rows(centre, (taps, inner))
    lane = iota((1, 128), 1)
    features = jnp.where(lane == 90, centre, jnp.where(lane == 91, number, features))
    pick = iota((8, frame_dev), 0)
    column = jnp.where(pick < 4, pick, frame_dev - 8 + pick)
    strip = dot((iota((8, frame_dev), 1) == column).astype(BF16), x.astype(BF16), ((1,), (1,)))
    lane = iota((8, 128), 1)
    repeat = (iota((rows, 128), 1) % rows == iota((rows, 128), 0)).astype(BF16)
    strip = jnp.where(lane // rows == iota((8, 128), 0), dot(strip.astype(BF16), repeat), 0.0)
    strip = jnp.sum(strip, axis=0, keepdims=True)

    def put(n, value):
        rows_out[pl.ds(n, devices, stride=FIRST), :] = jnp.broadcast_to(value, (devices, 128))

    near = jnp.concatenate([x[0:4], x[rows - 4 :]], axis=0)
    near = jnp.concatenate([near[:, :128], near[:, 128:]], axis=0)
    for d in range(devices):
        rows_out[FIRST * d : FIRST * d + 16, :] = near
    put(COLUMNS, strip)
    copies[2].wait()
    _, chan, many, half = own.shape
    share = share_of(devices, chan)
    holders = chan // share
    g = own[0].astype(F32)
    edges[0:chan] = g[:, 0, :]
    edges[chan:] = g[:, many - 1, :]

    def spread_out(v):
        if holders < devices:
            v = jnp.concatenate([v, jnp.zeros((devices - holders, 128), F32)], axis=0)
        return v

    for n in range(share):
        put(EDGES + n, spread_out(edges[n * holders : (n + 1) * holders, :]))
        put(EDGES + share + n, spread_out(edges[chan + n * holders : chan + (n + 1) * holders, :]))
    for n in range(2 * share, COLUMNS - EDGES):
        put(EDGES + n, jnp.zeros((1, 128), F32))
    end = iota((8, half), 0)
    at = iota((8, half), 1)
    ends = ((end == 0) & (at == 0)) | ((end == 1) & (at == half - 1))
    columns = dot(ends.astype(BF16), g.reshape(chan * many, half).astype(BF16), ((1,), (1,)))
    group = 128 // many
    source = iota((128, 128), 0)
    lane = iota((group, 128), 1)
    mine = lane // many == iota((group, 128), 0)
    parts = three_parts(features)
    for n in range(2):
        side = jnp.zeros((holders, 128), F32)
        for m in range(share):
            move = (iota((128, 128), 1) == SIDE + many * m + source % many).astype(BF16)
            first = m * holders * many // 128
            block = [columns[n : n + 1, 128 * q : 128 * (q + 1)] for q in range(first, first + holders * many // 128)]
            block = jnp.concatenate([jnp.where(mine, v, 0.0) for v in block], axis=0)
            side = side + dot(block.astype(BF16), move)
        put(SUMS + n, spread_out(side) + parts[n])
    put(SUMS + 2, parts[2])
    out[...] = rows_out[...].reshape(out.shape).astype(BF16)


def weights(own, bounds_hbm, k2_hbm, k1_hbm, gain_one_hbm, bias_one_hbm, gain_two_hbm, bias_two_hbm,
            wf, wb, w1, ws_hbm, pairs, singles, k1t, params, all_masks, edge_masks, twice, own_rows,
            k2, k1, vectors, bounds, ws, temp, sems):
    loads = start_all(
        (bounds_hbm, bounds),
        (k2_hbm, k2),
        (k1_hbm, k1),
        (gain_one_hbm, vectors.at[0]),
        (bias_one_hbm, vectors.at[1]),
        (gain_two_hbm, vectors.at[2]),
        (bias_two_hbm, vectors.at[3]),
        sems=sems,
    )
    _, many, count, half = own.shape
    temp[...] = own[0].astype(F32).reshape(many * count, half)
    for r in range(count):
        own_rows[r * many : (r + 1) * many] = temp[pl.ds(r, many, stride=count), :].astype(BF16)
    wait_all(loads)
    chan = k2.shape[1]
    span = wf.shape[1]
    taps = [k2[t].astype(F32) for t in range(9)]
    rest = jnp.zeros((chan, span - 9 * chan), F32)
    forward = jnp.concatenate(taps + [rest], axis=1)
    backward = jnp.concatenate([taps[8 - t].T for t in range(9)] + [rest], axis=1)
    for r in range(wb.shape[0] // chan):
        at = slice(r * chan, (r + 1) * chan)
        wb[at] = (pltpu.roll(backward, 3 * chan * r, 1) if r else backward).astype(BF16)
    full = jnp.concatenate([k1[n].astype(F32) for n in range(3)] + [jnp.zeros((7, chan), F32)], axis=0)
    low = [
        jnp.concatenate([full[3 * (2 - a) + 2 - b : 3 * (2 - a) + 3 - b] for a in range(3)], axis=1)
        for b in range(3)
    ]
    base = jnp.concatenate(low + [jnp.zeros((5, 3 * chan), F32)], axis=0)
    base = jnp.concatenate([base, jnp.zeros((8, ws.shape[1] - 3 * chan), F32)], axis=1)
    for m in range(ws.shape[0] // 8):
        ws[8 * m : 8 * m + 8] = (pltpu.roll(base, chan * m, 1) if m else base).astype(BF16)
    store_ws = pltpu.make_async_copy(ws, ws_hbm, sems.at[7])
    store_ws.start()
    count, frame_dev = all_masks.shape[0] // 3, all_masks.shape[1]
    frames = iota((count, frame_dev), 0) * frame_dev + iota((count, frame_dev), 1)
    for n, mask in enumerate(frame_masks(bounds, frames)):
        all_masks[n * count : (n + 1) * count] = mask
    q = iota(edge_masks.shape, 0)
    lane = iota(edge_masks.shape, 1)
    k = q % 8
    frames = (q // 8) * frame_dev + jnp.where(k < 4, k, k + frame_dev - 8)
    living, behind, ahead = frame_masks(bounds, frames)
    living = jnp.where((k == 0) | (k == 7), living, 0.0)
    edge_masks[...] = jnp.where(lane == 0, living, jnp.where(lane == 1, behind, jnp.where(lane == 2, ahead, 0.0)))
    params[...] = jnp.concatenate(
        [vectors[n] for n in range(4)] + [jnp.zeros((4, chan), F32)], axis=0
    )
    tap = iota((16, 128), 0)
    lane = iota((16, 128), 1)
    i = (tap * 11) >> 5
    ninth = (lane * 57) >> 9
    to_band = (lane == BAND * (tap - 3 * i) + i) & (tap < 9)
    to_left = (ninth == tap) & (tap < 9)
    to_right = (lane - 9 * ninth == tap) & (lane < 81)
    to_single = (lane == 81 + tap) & (tap < 9)
    source = iota((128, 128), 0) - 81
    lane = iota((128, 128), 1)
    ninth = (lane * 57) >> 9
    inside = (source >= 0) & (source < 9) & (lane < 81)
    twice[...] = jnp.where(inside, (source == ninth).astype(F32) + (source == lane - 9 * ninth).astype(F32), 0.0)
    for r in range(wf.shape[0] // chan):
        at = slice(r * chan, (r + 1) * chan)
        wf[at] = (pltpu.roll(forward, 3 * chan * r, 1) if r else forward).astype(BF16)
    k1t[...] = full
    k = full.astype(BF16)
    lanes = [dot(k, select.astype(BF16), ((0,), (0,))) for select in (to_band, to_left, to_right, to_single)]
    pairs[...] = lanes[1] * lanes[2]
    singles[...] = lanes[3]
    for m in range(w1.shape[0] // chan):
        w1[m * chan : (m + 1) * chan] = (pltpu.roll(lanes[0], m, 1) if m else lanes[0]).astype(BF16)
    store_ws.wait()


def feature_rows(centre, *parts):
    def folded(v):
        return jnp.sum(halves(v), axis=0, keepdims=True)

    rows = [jnp.zeros((1, 128), F32)] * 96
    for taps, weight in parts:
        z = [tap - centre for tap in taps]
        for s in range(9):
            left = z[s] * weight
            rows[81 + s] = rows[81 + s] + folded(left)
            for t in range(s, 9):
                rows[9 * s + t] = rows[9 * t + s] = rows[9 * s + t] + folded(left * z[t])
    return to_lanes(jnp.sum(jnp.concatenate(rows, axis=0), axis=1, keepdims=True))


def summed_blocks(ref, devices):
    block = ref.shape[0] // devices
    period = 8 // math.gcd(block, 8)
    step = period * block
    total = ref[0:step, :]
    for at in range(step, ref.shape[0], step):
        total = total + ref[at : at + step, :]
    result = total[0:block]
    for n in range(1, period):
        result = result + total[n * block : (n + 1) * block]
    return result


def moved_rows(v, step):
    if step == 0:
        return v
    count = v.shape[0]
    if abs(step) >= count:
        return jnp.zeros_like(v)
    zero = jnp.zeros((abs(step), v.shape[1]), v.dtype)
    if step > 0:
        return jnp.concatenate([zero, v[: count - step]], axis=0)
    return jnp.concatenate([v[-step:], zero], axis=0)


def silu_halves(h):
    t = jnp.tanh(h)
    one = 1.0 + t
    return h * one, one * (1.0 + h * (1.0 - t))


def forward_one(recv, spec, pairs, singles, twice, w1, wf, params, masks, all_masks, edge_masks,
                pre_two, payload, act, x3, stats, features_out, pre_one, got, strips, halo, rows_out):
    devices = recv.shape[0]
    n_mel, count = lax.axis_size("mel"), lax.axis_size("tm")
    rows = MEL_ROWS
    mels = n_mel * rows
    wide = masks.shape[1]
    frame_dev = wide - RIM
    chan = params.shape[1]
    me_m, me_t = lax.axis_index("mel"), lax.axis_index("tm")
    usable, behind, ahead = (masks[n : n + 1] for n in range(3))
    total = masks[3:4, 0:1]
    got[...] = recv[...].astype(F32).reshape(devices * FIRST, 128)

    def every(n):
        return got[pl.ds(n, devices, stride=FIRST), :]

    lane = iota((count, 128), 1)
    bands = [got[pl.ds(FIRST * k * count + COLUMNS, count, stride=FIRST), :] for k in range(n_mel)]
    for c in range(8):
        column = jnp.zeros((count, 128), F32)
        for k, band in enumerate(bands):
            part = jnp.where(lane // rows == c, band, 0.0)
            column = column + (pltpu.roll(part, rows * (k - c) % 128, 1) if k != c else part)
        strips[pl.ds(c, count, stride=8), :] = column
    at = pl.multiple_of(FIRST * (jnp.maximum(me_m - 1, 0) * count + me_t), 8)
    above = got[pl.ds(at, 16), :] * (me_m > 0).astype(F32)
    at = pl.multiple_of(FIRST * (jnp.minimum(me_m + 1, n_mel - 1) * count + me_t), 8)
    below = got[pl.ds(at, 16), :] * (me_m < n_mel - 1).astype(F32)
    above = jnp.concatenate([above[4:8], above[12:16]], axis=1)
    below = jnp.concatenate([below[0:4], below[8:12]], axis=1)
    own = spec[0].astype(F32) * usable[:, :frame_dev]
    at = pl.multiple_of(8 * jnp.minimum(me_t + 1, count - 1), 8)
    after = strips[pl.ds(at, 8), :][:, :mels] * (me_t + 1 < count).astype(F32)
    at = pl.multiple_of(8 * jnp.maximum(me_t - 1, 0), 8)
    before = strips[pl.ds(at, 8), :][:, :mels] * (me_t > 0).astype(F32)
    sides = jnp.concatenate([after[0:4], before[4:8], jnp.zeros((8, mels), F32)], axis=0).astype(BF16)
    side = iota((16, RIM), 0)
    place = iota((16, RIM), 1) == jnp.where(side < 4, side, jnp.where(side < 8, side + RIM - 8, -1))
    halo[0:8] = jnp.zeros((8, RIM), F32)
    halo[mels : mels + 8] = jnp.zeros((8, RIM), F32)
    halo[4 : mels + 4] = dot(sides, place.astype(BF16), ((0,), (0,)))
    rim = halo[pl.ds(pl.multiple_of(me_m * rows, 8), BAND), :]
    near = jnp.concatenate([jnp.concatenate([above, own, below], axis=0), rim], axis=1)
    x3[...] = jnp.concatenate(
        [
            pltpu.roll(near, 1, 1) * behind,
            near,
            pltpu.roll(near, wide - 1, 1) * ahead,
            jnp.broadcast_to(usable, (BAND, wide)),
            jnp.zeros((128 - 4 * BAND, wide), F32),
        ],
        axis=0,
    ).astype(BF16)
    pre_one[...] = dot(w1[...], x3[...])
    lane = iota((1, 128), 1)
    parts = jnp.where(lane < 92, every(SUMS) + every(SUMS + 1) + every(SUMS + 2), 0.0)
    centres, numbers = parts[:, 90:91], parts[:, 91:92]
    centre = jnp.sum(centres * numbers, axis=0, keepdims=True)
    centre = centre / jnp.maximum(jnp.sum(numbers, axis=0, keepdims=True), 1.0)
    delta = centres - centre
    features = jnp.sum(parts + delta * numbers * jnp.where(lane < 81, delta, 1.0), axis=0, keepdims=True)
    moved = jnp.sum(delta * parts, axis=0, keepdims=True)
    def edge_row(k, n):
        first = FIRST * k * count + n
        return jnp.concatenate(
            [got[pl.ds(first, count, stride=FIRST), :], got[pl.ds(first + 8, count, stride=FIRST), :]], axis=1
        )

    edge_rows = [[edge_row(k, n) for n in (0, 1, 6, 7)] for k in range(n_mel)]
    zero = jnp.zeros((count, frame_dev), F32)
    rows_of = [[], [], []]
    for k, (top, second, fore, bottom) in enumerate(edge_rows):
        for n, v in enumerate((edge_rows[k - 1][3] if k else zero, top, second)):
            rows_of[n].append(v)
        for n, v in enumerate((fore, bottom, edge_rows[k + 1][0] if k + 1 < n_mel else zero)):
            rows_of[n].append(v)
    f_usable, f_behind, f_ahead = (all_masks[n * count : (n + 1) * count, :] for n in range(3))
    lane = iota((count, frame_dev), 1)

    def frame_before(v):
        v = pltpu.roll(v, 1, 1)
        return jnp.where(lane == 0, pltpu.roll(v, 1, 0), v) * f_behind

    def frame_after(v):
        v = pltpu.roll(v, frame_dev - 1, 1)
        return jnp.where(lane == frame_dev - 1, pltpu.roll(v, count - 1, 0), v) * f_ahead

    taps = []
    for group in rows_of:
        for move in (frame_before, lambda v: v, frame_after):
            taps.append(jnp.concatenate([move(v) for v in group], axis=1))
    f_usable = jnp.concatenate([f_usable] * (2 * n_mel), axis=1)
    borders = (taps, f_usable)
    edge = strips[...]
    q_usable, q_behind, q_ahead = (edge_masks[:, n : n + 1] for n in range(3))
    lane = iota((count * 8, 128), 1)
    inside = (lane < mels) & (lane % rows != 0) & (lane % rows != rows - 1)
    shifted = [
        pltpu.roll(edge, 1, 0) * q_behind,
        edge,
        pltpu.roll(edge, count * 8 - 1, 0) * q_ahead,
    ]
    taps = [pltpu.roll(v, (1 - i) % 128, 1) if i != 1 else v for i in range(3) for v in shifted]
    features = features + feature_rows(centre, borders, (taps, jnp.where(inside, q_usable, 0.0)))
    features = jnp.where(iota((1, 128), 1) < 90, features, 0.0)
    near_mean = jnp.sum(singles[...] * features, axis=1, keepdims=True) / total
    around = jnp.sum(singles[...], axis=1, keepdims=True)
    square = jnp.sum(pairs[...] * features, axis=1, keepdims=True)
    square = (square + 2.0 * around * jnp.sum(singles[...] * moved, axis=1, keepdims=True)) / total
    inv = lax.rsqrt(square - near_mean * near_mean + 1e-05)
    mean = near_mean + centre * around
    lane = iota((chan, 128), 1)
    stats[0:chan] = jnp.where(lane == 0, mean, jnp.where(lane == 1, inv, 0.0))
    stats[chan : chan + 8] = jnp.broadcast_to(to_lanes(near_mean), (8, 128))
    stats[chan + 8 : chan + 16] = jnp.broadcast_to(to_lanes(inv), (8, 128))
    scale = 0.5 * to_column(params[0:1], chan) * inv
    shift = 0.5 * to_column(params[1:2], chan) - mean * scale
    stats[chan + 16 :] = jnp.where(lane == 0, scale, jnp.where(lane == 1, shift, 0.0))
    scale = jnp.broadcast_to(scale, (chan, wide))
    shift = jnp.broadcast_to(shift, (chan, wide))
    ext = w1.shape[0] // chan
    block, taps = wf.shape
    first = jnp.zeros((chan, 128), F32)
    second = jnp.zeros((chan, 128), F32)
    own_mask = usable[:, :frame_dev]
    low_masks = [m.astype(BF16) for m in (usable, behind, ahead)]
    for r in range(ext):
        value, _ = silu_halves(pre_one[r * chan : (r + 1) * chan, :] * scale + shift)
        if not 0 <= r - 3 < rows:
            value = value * row_valid(r - 3, rows)
        base = r * 3 * chan
        low = value.astype(BF16) * low_masks[0]
        act[base : base + chan, :], act[base + 2 * chan : base + 3 * chan, :] = shifted_frames(low, *low_masks[1:])
        act[base + chan : base + 2 * chan, :] = low
        if r < 3 or r % 2 == 0:
            continue
        g = (r - 3) // 2
        result = dot(wf[...], act[g * 3 * block : g * 3 * block + taps, :])
        pre_two[g * block : (g + 1) * block] = result
        for q in range(2):
            if 2 <= 2 * g + q < rows + 2:
                p = result[q * chan : (q + 1) * chan, :frame_dev]
                masked = p * own_mask
                first = first + halves(masked)
                second = second + halves(masked * p)
    moved = dot(jnp.broadcast_to(moved, (8, 128)), twice[...], precision=EXACT)[0:1]
    features_out[...] = jnp.concatenate(
        [features + moved, jnp.broadcast_to(centre, (1, 128)), jnp.zeros((6, 128), F32)], axis=0
    )
    share = share_of(devices, chan)

    def put(n, value):
        rows_out[pl.ds(n, devices, stride=SECOND), :] = jnp.broadcast_to(value, (devices, 128))

    for n in range(share):
        put(3 + n, moved_rows(every(EDGES + share + n), count))
        put(3 + share + n, moved_rows(every(EDGES + n), -count))
    for n in range(3 + 2 * share, SECOND - 1):
        put(n, jnp.zeros((1, 128), F32))
    lane = iota((devices, 128), 1)
    tm = iota((devices, 128), 0) % count
    lefts = jnp.where(lane >= SIDE, every(SUMS), 0.0)
    rights = jnp.where(lane >= SIDE, every(SUMS + 1), 0.0)
    beside = jnp.zeros((devices, 128), F32)
    for n, step in enumerate((0, count, -count)):
        one = jnp.where(tm > 0, moved_rows(rights, step + 1), 0.0)
        two = jnp.where(tm < count - 1, moved_rows(lefts, step - 1), 0.0)
        beside = beside + pltpu.roll(one, (32 * n - SIDE) % 128, 1) + pltpu.roll(two, (32 * n + 16 - SIDE) % 128, 1)
    put(SECOND - 1, beside)
    first = jnp.sum(first, axis=1, keepdims=True)
    second = jnp.sum(second, axis=1, keepdims=True)
    for n, part in enumerate(three_parts(to_lanes(first) + to_lanes(second, chan))):
        put(n, part)
    payload[...] = rows_out[...].reshape(payload.shape).astype(BF16)


def sum_rows(devices, taps):
    return -(-taps // devices) + 2


def backward_scaled(recv, pre_two, act, own_rows, params, masks,
                    grad, payload, pairs, stats, sides, up, right, got, beyond):
    devices = recv.shape[0]
    got[...] = recv[...].astype(F32).reshape(devices * SECOND, 128)
    chan = params.shape[1]
    half = own_rows.shape[1]
    lane = iota((half, 2 * half), 1)
    spread = jnp.where(lane >> 1 == iota((half, 2 * half), 0), 0.25, 0.0).astype(BF16)
    rows = MEL_ROWS
    wide = pre_two.shape[1]
    frame_dev = wide - RIM
    usable = masks[0:1]
    share = share_of(devices, chan)
    holders = chan // share

    def every(n):
        return got[pl.ds(n, devices, stride=SECOND), :]

    beside = every(SECOND - 1)[:holders]
    lane = iota((holders, RIM), 1)
    many = rows // 2
    up[0 : many * chan] = dot(own_rows[...], spread)
    for n in range(share):
        first = n * holders
        beyond[first : first + holders, :] = every(3 + n)[:holders]
        beyond[chan + first : chan + first + holders, :] = every(3 + share + n)[:holders]
        for r in range(many + 2):
            at = many * n + (r if r < many else 32 + many - 1 if r == many else 64)
            left, right_of = beside[:, at : at + 1], beside[:, at + 16 : at + 17]
            side = jnp.where(lane >= RIM - 2, 0.25 * left, jnp.where(lane < 2, 0.25 * right_of, 0.0))
            sides[r * chan + first : r * chan + first + holders, :] = side
    up[many * chan :] = dot(beyond[...].astype(BF16), spread)
    total = masks[3:4, 0:1]
    sums = jnp.sum(every(0) + every(1) + every(2), axis=0, keepdims=True)
    mean = to_column(sums, chan) / total
    inv = lax.rsqrt(to_column(sums, chan, chan) / total - mean * mean + 1e-05)
    lane = iota((chan, 128), 1)
    scale = 0.5 * to_column(params[2:3], chan) * inv
    shift = 0.5 * to_column(params[3:4], chan) - mean * scale
    columns = jnp.zeros((chan, 128), F32)
    for n, column in enumerate((mean, inv, scale, shift)):
        columns = jnp.where(lane == n, column, columns)
    stats[0:chan] = columns
    stats[chan : chan + 8] = jnp.broadcast_to(to_lanes(inv), (8, 128))
    shift = jnp.broadcast_to(shift, (chan, wide))
    scale = jnp.broadcast_to(scale, (chan, wide))
    mean = jnp.broadcast_to(mean, (chan, frame_dev))
    inv = jnp.broadcast_to(inv, (chan, frame_dev))
    first = jnp.zeros((chan, 128), F32)
    second = jnp.zeros((chan, 128), F32)
    own_mask = usable[:, :frame_dev]
    right[3 * chan :] = jnp.ones((16, rows * frame_dev), BF16)
    table = jnp.zeros((9 * chan, 3 * chan + 16), F32)
    for q in list(range(2, rows + 2)) + [0, 1, rows + 2, rows + 3]:
        r = q // 2
        at = slice(q * chan, (q + 1) * chan)
        m = q - 2
        mask = 0.5 * usable if 0 <= m < rows else usable * (0.5 * row_valid(m, rows))
        if q % 2 == 0:
            spot = (r - 1 if 1 <= r <= many else many + (r > 0)) * chan
            upstream = jnp.concatenate([up[spot : spot + chan, :], sides[spot : spot + chan, :]], axis=1)
        pre = pre_two[at, :]
        value, slope = silu_halves(pre * scale + shift)
        g = upstream * slope * mask
        grad[at, :] = g
        if not 0 <= m < rows:
            continue
        g = g[:, :frame_dev]
        normed = (pre[:, :frame_dev] - mean) * inv
        first = first + halves(g * normed)
        second = second + halves(g)
        value = value[:, :frame_dev] * own_mask
        both = value if m % 2 == 0 else both + value
        if m % 2:
            pairs[(r - 1) * chan : r * chan, :] = both
        lanes = slice(m * frame_dev, (m + 1) * frame_dev)
        right[0:chan, lanes] = g.astype(BF16)
        right[chan : 2 * chan, lanes] = normed.astype(BF16)
        right[2 * chan : 3 * chan, lanes] = (g - right[0:chan, lanes].astype(F32)).astype(BF16)
        if m in (5, 11, rows - 1):
            start = m - m % 6
            left = [act[(n + 2) * 3 * chan : (n + 5) * 3 * chan, :frame_dev] for n in range(start, m + 1)]
            lanes = slice(start * frame_dev, (m + 1) * frame_dev)
            table = table + dot(jnp.concatenate(left, axis=1), right[:, lanes], ((1,), (1,)))
    first = jnp.sum(first, axis=1, keepdims=True)
    second = jnp.sum(second, axis=1, keepdims=True)
    totals = to_lanes(first) + to_lanes(second, chan)
    block = payload.shape[0] // devices
    payload[pl.ds(0, devices, stride=block), :] = jnp.broadcast_to(totals, (devices, 128))
    rest = jnp.concatenate([table[:, 2 * chan :], jnp.zeros((9 * chan, chan - 16), F32)], axis=1)
    both = table[:, : 2 * chan] + jnp.where(iota(rest.shape, 1) < chan, rest, 0.0)
    single = rest[:, chan : chan + 1]
    lane = iota((devices, 128), 1)
    constants = jnp.zeros((devices, 128), F32)
    for k in range(block - 2):
        cut, ones = both[k * devices : (k + 1) * devices], single[k * devices : (k + 1) * devices]
        short = devices - cut.shape[0]
        if short:
            cut = jnp.concatenate([cut, jnp.zeros((short, 128), F32)], axis=0)
            ones = jnp.concatenate([ones, jnp.zeros((short, 1), F32)], axis=0)
        payload[pl.ds(1 + k, devices, stride=block), :] = cut
        constants = jnp.where(lane == k, ones, constants)
    payload[pl.ds(block - 1, devices, stride=block), :] = constants


def pool(totals, pairs, out, gain_out, bias_out, temp):
    gain_out[...] = totals[0:1, : gain_out.shape[1]]
    bias_out[...] = totals[0:1, gain_out.shape[1] :]
    chan, rows, half = out.shape[1:]
    to_mean = jnp.where(iota((2 * half, half), 0) >> 1 == iota((2 * half, half), 1), 0.25, 0.0)
    pooled = dot(pairs[...], to_mean, precision=EXACT)
    for r in range(rows):
        temp[pl.ds(r, chan, stride=rows), :] = pooled[r * chan : (r + 1) * chan]
    out[0] = temp[...].reshape(chan, rows, half).astype(BF16)


def backward(recv, pre_two, grad, stats_two, w1, x3, stats, params, masks, wb,
             out, own_low, payload, totals, g3, pre_one, g1):
    chan = params.shape[1]
    rows = MEL_ROWS
    wide = pre_two.shape[1]
    frame_dev = wide - RIM
    usable = masks[0:1]
    behind, ahead = (masks[n : n + 1].astype(BF16) for n in (1, 2))
    total = masks[3:4, 0:1]
    devices = payload.shape[0] // 14
    pre_one[...] = dot(w1[3 * chan : (rows + 3) * chan], x3[:, :frame_dev])

    received = summed_blocks(recv, devices)
    sums = received[0:1]
    gain_sum, bias_sum = sums[:, :chan], sums[:, chan:]
    totals[...] = jnp.broadcast_to(sums, (8, 128))
    mean, inv = stats_two[0:chan, 0:1], stats_two[0:chan, 1:2]
    factor = to_column(params[2:3], chan) * inv
    gain_part = factor * (to_column(sums, chan) / total * inv)
    bias_part = factor * (to_column(sums, chan, chan) / total) - mean * gain_part
    gain_part = jnp.broadcast_to(gain_part, (chan, wide))
    bias_part = jnp.broadcast_to(bias_part, (chan, wide))
    factor = jnp.broadcast_to(factor, (chan, wide))
    scale = jnp.broadcast_to(stats[chan + 16 :, 0:1], (chan, frame_dev))
    shift = jnp.broadcast_to(stats[chan + 16 :, 1:2], (chan, frame_dev))
    factor_one = jnp.broadcast_to(to_column(params[0:1], chan) * stats[0:chan, 1:2], (chan, frame_dev))
    own_mask = 0.5 * usable[:, :frame_dev]
    count = pre_two.shape[0] // chan
    table = jnp.zeros((chan, 128), F32)

    def tap_sums(m):
        part = g1[m * chan : (m + 4) * chan, :]
        high = lax.reduce_precision(part, 8, 7)
        low = (part - high).astype(BF16)
        taps_in = x3[:, :frame_dev]
        products = dot(high.astype(BF16), taps_in, ((1,), (1,))) + dot(low, taps_in, ((1,), (1,)))
        moved = [pltpu.roll(products[k * chan : (k + 1) * chan], 128 - (m + k + 3), 1) for k in range(4)]
        return (moved[0] + moved[1]) + (moved[2] + moved[3])

    for q in range(count):
        at = slice(q * chan, (q + 1) * chan)
        mask = usable if 0 <= q - 2 < rows else usable * row_valid(q - 2, rows)
        low = (factor * grad[at, :] - (bias_part + pre_two[at, :] * gain_part) * mask).astype(BF16)
        out[at, :] = low
        if not 1 <= q < count - 1:
            continue
        base = (q - 1) * 3 * chan
        for n, v in enumerate((low,) + shifted_frames(low, behind, ahead)):
            spot = base + (1, 0, 2)[n] * chan
            g3[spot : spot + chan, :] = v[:, :frame_dev]
        start = q - 4
        if start < 0 or start % 2:
            continue
        result = dot(wb[...], g3[start * 3 * chan : (start + 4) * 3 * chan, :])
        for n in range(2):
            m = start + n
            at = slice(m * chan, (m + 1) * chan)
            _, slope = silu_halves(pre_one[at, :] * scale + shift)
            value = result[n * chan : (n + 1) * chan] * slope * own_mask
            own_low[at, :] = (value * factor_one).astype(BF16)
            g1[at, :] = value
        if start % 4 == 2 and start > 2:
            table = table + tap_sums(start - 6)
    table = table + tap_sums(rows - 4)
    tap = iota((16, 128), 0)
    lane = iota((16, 128), 1)
    i = (tap * 11) >> 5
    select = ((lane == BAND * (tap - 3 * i) + i) & (tap < 9)) | ((lane == 3 * BAND) & (tap == 9))
    rows10 = dot(select.astype(F32), table, ((1,), (1,)), EXACT)
    share = received.shape[0] - 2
    mine = received[1 : share + 1]
    single = to_column(received[share + 1 :], share)
    factor_l = params[2:3] * stats_two[chan : chan + 1, :chan]
    mine = mine[:, :chan] - (bias_sum * single + gain_sum * mine[:, chan:]) / total
    mine = factor_l * mine
    lower = -(-share // 2)
    mine = jnp.concatenate([mine] + [jnp.zeros((2 * lower - share, chan), F32)] * (share % 2), axis=0)
    mine = jnp.concatenate([mine[:lower], mine[lower:]], axis=1)
    if lower < 9:
        mine = jnp.concatenate([mine, jnp.zeros((9 - lower, 128), F32)], axis=0)
    sums = jnp.concatenate([rows10[0:5], rows10[5:10]], axis=1)
    block = jnp.concatenate([sums, mine], axis=0)
    block = jnp.concatenate([block] * 4, axis=0)
    for d in range(0, devices, 4):
        payload[14 * d : 14 * (d + 4), :] = block


def transposed(grad, own_low, w1, wb, x3, stats, params, masks, ws_hbm, first, normed, ws, low, g3, rim, sem):
    load = pltpu.make_async_copy(ws_hbm, ws, sem)
    load.start()
    rows = MEL_ROWS
    chan = own_low.shape[0] // rows
    wide = grad.shape[1]
    frame_dev = wide - RIM
    count = grad.shape[0] // chan
    usable = masks[0:1]
    behind, ahead = (masks[n : n + 1].astype(BF16) for n in (1, 2))
    mean = jnp.broadcast_to(stats[0:chan, 0:1], (chan, wide))
    inv = jnp.broadcast_to(stats[0:chan, 1:2], (chan, wide))
    scale = jnp.broadcast_to(stats[chan + 16 :, 0:1], (chan, wide))
    shift = jnp.broadcast_to(stats[chan + 16 :, 1:2], (chan, wide))
    factor = jnp.broadcast_to(to_column(params[0:1], chan) * stats[0:chan, 1:2], (chan, wide))
    edge = (0, 1, 2, 3, count - 4, count - 3, count - 2, count - 1)
    for q in range(count):
        value = grad[q * chan : (q + 1) * chan, :]
        for n, v in enumerate((value,) + shifted_frames(value, behind, ahead)):
            spot = (3 * q + (1, 0, 2)[n]) * chan
            rim[spot : spot + chan, :] = v[:, frame_dev:]
            if q in edge:
                spot = (3 * edge.index(q) + (1, 0, 2)[n]) * chan
                g3[spot : spot + chan, :] = v[:, :frame_dev]
    low[chan : (rows + 1) * chan, :frame_dev] = own_low[...]

    def put(m, lanes, result, pre_one):
        at = slice((m + 1) * chan, (m + 2) * chan)
        _, slope = silu_halves(pre_one * scale[:, lanes] + shift[:, lanes])
        mask = usable[:, lanes] * (0.5 * row_valid(m, rows))
        low[at, lanes] = (result * slope * mask * factor[:, lanes]).astype(BF16)

    pre_one = dot(w1[2 * chan : (rows + 4) * chan, :], x3[...])
    for m in range(rows + 2):
        at = slice(m * chan, (m + 1) * chan)
        mask = usable * row_valid(m - 1, rows)
        normed[at, :] = ((pre_one[at] - mean) * inv * mask).astype(BF16)
    beside = slice(frame_dev, wide)
    for start in range(0, rows + 2, 2):
        result = dot(wb[...], rim[start * 3 * chan : (start + 4) * 3 * chan, :])
        for n in range(2):
            at = slice((start + n) * chan, (start + n + 1) * chan)
            put(start + n - 1, beside, result[n * chan : (n + 1) * chan], pre_one[at, frame_dev:])
    own = slice(0, frame_dev)
    result = dot(wb[...], g3[: 4 * 3 * chan, :])
    put(-1, own, result[:chan], pre_one[:chan, :frame_dev])
    result = dot(wb[...], g3[4 * 3 * chan :, :])
    put(rows, own, result[chan:], pre_one[(rows + 1) * chan :, :frame_dev])
    load.wait()
    first[...] = dot(ws[...], low[...])


def finish(recv, features, stats, k1t, first, normed, ws, params, masks,
           spec_hbm, kernel_one_hbm, kernel_two_hbm, gain_hbm, bias_hbm,
           table, spec_grad, kernel_one, kernel_two, gain_out, bias_out, sems):
    chan = params.shape[1]
    rows = MEL_ROWS
    wide = normed.shape[1]
    frame_dev = wide - RIM
    usable, behind, ahead = (masks[n : n + 1] for n in range(3))
    total = masks[3:4, 0:1]
    gain = params[0:1]
    count = recv.shape[0] // 14
    share = -(-9 * chan // count)
    lower = -(-share // 2)
    left = [recv[pl.ds(5 + p, count, stride=14), :] for p in range(lower)]
    whole = jnp.concatenate([v[:, :chan] for v in left] + [v[:, chan:] for v in left], axis=0)
    for t in range(9):
        kernel_two[t] = whole[t * chan : (t + 1) * chan].T
    stores = [pltpu.make_async_copy(kernel_two, kernel_two_hbm, sems.at[3])]
    stores[0].start()
    sums = summed_blocks(recv, count)[0:5]
    ten = jnp.concatenate([sums[:, :chan], sums[:, chan:]], axis=0)
    bias_sum = ten[9:10]
    mean_l, inv_l = stats[chan : chan + 1, :chan], stats[chan + 8 : chan + 9, :chan]
    ten = ten - features[1:2, 0:1] * bias_sum
    k = k1t[0:9]
    gain_sum = inv_l * (jnp.sum(k * ten[0:9], axis=0, keepdims=True) - mean_l * bias_sum)
    gain_out[...] = gain_sum
    bias_out[...] = bias_sum
    for n, (source, target) in enumerate(((gain_out, gain_hbm), (bias_out, bias_hbm))):
        stores.append(pltpu.make_async_copy(source, target, sems.at[n]))
        stores[-1].start()
    factor_l = gain * inv_l
    scale = factor_l * gain_sum / total
    scale = jnp.concatenate([scale, scale], axis=1)
    scale = jnp.concatenate([scale] * ((rows + 2) // 2), axis=1)
    taps = first[...] - dot((ws[...].astype(F32) * scale).astype(BF16), normed[...])
    for part in range(wide // 128):
        table[part] = taps[:, 128 * part : 128 * (part + 1)]
    moved = [
        jnp.concatenate([table[part, pl.ds(b, rows, stride=8), :] for part in range(wide // 128)], axis=1)
        for b in range(3)
    ]
    constant = jnp.sum(k * (factor_l * bias_sum / total), axis=1, keepdims=True)
    for a in range(3):
        row = iota((rows, 1), 0) + (a - 1) + lax.axis_index("mel") * rows
        valid = ((row >= 0) & (row < lax.axis_size("mel") * rows)).astype(F32) * usable
        for b in range(3):
            t = 3 * (2 - a) + 2 - b
            moved[b] = moved[b] - constant[t : t + 1] * valid
    result = pltpu.roll(moved[0], 1, 1) * behind + moved[1] + pltpu.roll(moved[2], wide - 1, 1) * ahead
    spec_grad[0] = (result * usable)[:, :frame_dev]
    stores.append(pltpu.make_async_copy(spec_grad, spec_hbm, sems.at[2]))
    stores[-1].start()
    row = features[0:1, :]
    lane = iota((1, 128), 1)
    gram = jnp.concatenate(
        [jnp.where(lane < 9, pltpu.roll(row, 128 - 9 * t, 1) if t else row, 0.0) for t in range(9)]
        + [jnp.zeros((7, 128), F32)],
        axis=0,
    )
    single = to_column(row, 16, 81)[0:9]
    k_rows = jnp.concatenate([k1t[...], jnp.zeros((112, chan), F32)], axis=0)
    normed_taps = inv_l * (dot(gram, k_rows, precision=EXACT)[0:9] - single * mean_l)
    grad_taps = factor_l * (ten[0:9] - (bias_sum * single + gain_sum * normed_taps) / total)
    for i in range(3):
        kernel_one[i] = grad_taps[3 * i : 3 * i + 3]
    stores.append(pltpu.make_async_copy(kernel_one, kernel_one_hbm, sems.at[4]))
    stores[-1].start()
    for store in stores:
        store.wait()


def run(kernel, outs, scratch, *args, hbm=0, apart=(), flops=10**8, size=4 * 10**6):
    vmem = pl.BlockSpec(memory_space=pltpu.VMEM)
    devices = lax.axis_size("mel") * lax.axis_size("tm")
    specs = []
    args = list(args)
    for n, a in enumerate(args):
        if hbm and n >= len(args) - hbm:
            specs.append(pl.BlockSpec(memory_space=pltpu.HBM))
            args[n] = pltpu.with_memory_space_constraint(a, pltpu.HBM)
        else:
            specs.append(vmem)
            args[n] = pltpu.with_memory_space_constraint(a, pltpu.VMEM)
    return pl.pallas_call(
        kernel,
        out_shape=outs,
        in_specs=specs,
        out_specs=[pl.BlockSpec(memory_space=pltpu.HBM) if n in apart else vmem for n in range(len(outs))],
        scratch_shapes=scratch,
        compiler_params=pltpu.CompilerParams(vmem_limit_bytes=(29 + devices // 32) * 2**20),
        cost_estimate=pl.CostEstimate(flops=flops, bytes_accessed=size, transcendentals=0),
    )(*args)


def shape(dims, dtype=F32):
    return jax.ShapeDtypeStruct(dims, dtype)


def kept(dims, dtype=F32):
    return pltpu.VMEM(dims, dtype)


def far(dims, dtype=F32):
    return pltpu.HBM(dims, dtype)


def exchange(blocks, axes=AXES):
    return lax.all_to_all(blocks, axes, 0, 0, tiled=True)


def exchange_rows(rows, axes=AXES):
    return exchange(rows[:, None, :], axes)[:, 0, :]


def shards(spectrum, clip_bounds, kernel_one, gain_one, bias_one, kernel_two, gain_two, bias_two, pooled_grad):
    _, rows, frame_dev = spectrum.shape
    chan = kernel_two.shape[0]
    n_mel, n_tm = lax.axis_size("mel"), lax.axis_size("tm")
    devices = n_mel * n_tm
    half = frame_dev // 2
    wide = frame_dev + RIM
    mels = n_mel * rows

    packed, own, spec, masks = run(
        pack,
        [
            kept((devices, FIRST, 128), BF16),
            kept(pooled_grad.shape, BF16),
            kept(spectrum.shape, BF16),
            kept((8, wide)),
        ],
        [
            pltpu.SMEM(clip_bounds.shape, jnp.int32),
            pltpu.VMEM((2 * chan, half), F32),
            pltpu.VMEM((devices * FIRST, 128), F32),
            pltpu.SemaphoreType.DMA((3,)),
        ],
        spectrum,
        pooled_grad,
        clip_bounds,
        hbm=3,
    )
    recv = exchange(packed)
    ext = rows + 6
    span = 4 * 3 * chan
    wf, wb, w1, ws, pairs, singles, k1t, params, all_masks, edge_masks, twice, own_rows = run(
        weights,
        [
            kept((2 * chan, span), BF16),
            kept((2 * chan, span), BF16),
            kept((ext * chan, 128), BF16),
            far((rows * 8, (rows + 2) * chan), BF16),
            kept((chan, 128)),
            kept((chan, 128)),
            kept((16, chan)),
            kept((8, chan)),
            kept((3 * n_tm, frame_dev)),
            kept((n_tm * 8, 128)),
            kept((128, 128)),
            kept((chan * rows // 2, half), BF16),
        ],
        [
            pltpu.VMEM((9, chan, chan), BF16),
            pltpu.VMEM((3, 3, chan), BF16),
            pltpu.VMEM((4, 1, chan), F32),
            pltpu.SMEM(clip_bounds.shape, jnp.int32),
            pltpu.VMEM((rows * 8, (rows + 2) * chan), BF16),
            pltpu.VMEM((chan * rows // 2, half), F32),
            pltpu.SemaphoreType.DMA((8,)),
        ],
        own,
        clip_bounds,
        jnp.transpose(kernel_two, (2, 3, 0, 1)).reshape(9, chan, chan),
        jnp.transpose(kernel_one, (1, 2, 0)),
        gain_one[None],
        bias_one[None],
        gain_two[None],
        bias_two[None],
        hbm=7,
        apart=(3,),
    )
    pre_two, payload, act, x3, stats_one, features = run(
        forward_one,
        [
            kept(((rows + 4) * chan, wide)),
            kept((devices, SECOND, 128), BF16),
            kept((ext * 3 * chan, wide), BF16),
            kept((128, wide), BF16),
            kept((2 * chan + 16, 128)),
            kept((8, 128)),
        ],
        [
            pltpu.VMEM((ext * chan, wide), F32),
            pltpu.VMEM((devices * FIRST, 128), F32),
            pltpu.VMEM((n_tm * 8, 128), F32),
            pltpu.VMEM((mels + 8, RIM), F32),
            pltpu.VMEM((devices * SECOND, 128), F32),
        ],
        recv,
        spec,
        pairs,
        singles,
        twice,
        w1,
        wf,
        params,
        masks,
        all_masks,
        edge_masks,
    )
    recv = exchange(payload)
    grad, payload, row_pairs, stats_two = run(
        backward_scaled,
        [
            kept(((rows + 4) * chan, wide)),
            kept((devices * sum_rows(devices, 9 * chan), 128)),
            kept((rows // 2 * chan, frame_dev)),
            kept((chan + 8, 128)),
        ],
        [
            pltpu.VMEM(((rows // 2 + 2) * chan, RIM), F32),
            pltpu.VMEM(((rows // 2 + 2) * chan, frame_dev), F32),
            pltpu.VMEM((3 * chan + 16, rows * frame_dev), BF16),
            pltpu.VMEM((devices * SECOND, 128), F32),
            pltpu.VMEM((2 * chan, half), F32),
        ],
        recv,
        pre_two,
        act,
        own_rows,
        params,
        masks,
    )
    recv = exchange_rows(payload)
    grad, own_low, payload, totals = run(
        backward,
        [
            kept(((rows + 4) * chan, wide), BF16),
            kept((rows * chan, frame_dev), BF16),
            kept((devices * 14, 128)),
            kept((8, 128)),
        ],
        [
            pltpu.VMEM(((rows + 2) * 3 * chan, frame_dev), BF16),
            pltpu.VMEM((rows * chan, frame_dev), F32),
            pltpu.VMEM((rows * chan, frame_dev), F32),
        ],
        recv,
        pre_two,
        grad,
        stats_two,
        w1,
        x3,
        stats_one,
        params,
        masks,
        wb,
    )
    recv = exchange_rows(payload)
    pooled, gain_two_grad, bias_two_grad = run(
        pool,
        [shape((1, chan, rows // 2, half), BF16), shape((1, chan)), shape((1, chan))],
        [
            pltpu.VMEM((rows // 2 * chan, 128), F32),
        ],
        totals,
        row_pairs,
    )
    first, normed, ws = run(
        transposed,
        [
            kept((rows * 8, wide)),
            kept(((rows + 2) * chan, wide), BF16),
            kept((rows * 8, (rows + 2) * chan), BF16),
        ],
        [
            pltpu.VMEM(((rows + 2) * chan, wide), BF16),
            pltpu.VMEM((8 * 3 * chan, frame_dev), BF16),
            pltpu.VMEM(((rows + 4) * 3 * chan, RIM), BF16),
            pltpu.SemaphoreType.DMA,
        ],
        grad,
        own_low,
        w1,
        wb,
        x3,
        stats_one,
        params,
        masks,
        ws,
        hbm=1,
    )
    spec_grad, kernel_one_grad, kernel_two_grad, gain_one_grad, bias_one_grad = run(
        finish,
        [
            shape((1, rows, frame_dev)),
            shape((3, 3, chan)),
            shape((9, chan, chan)),
            shape((1, chan)),
            shape((1, chan)),
        ],
        [
            pltpu.VMEM((3, rows * 8, 128), F32),
            pltpu.VMEM((1, rows, frame_dev), F32),
            pltpu.VMEM((3, 3, chan), F32),
            pltpu.VMEM((9, chan, chan), F32),
            pltpu.VMEM((1, chan), F32),
            pltpu.VMEM((1, chan), F32),
            pltpu.SemaphoreType.DMA((5,)),
        ],
        recv,
        features,
        stats_one,
        k1t,
        first,
        normed,
        ws,
        params,
        masks,
        apart=range(5),
    )
    kernel_two_grad = jnp.transpose(kernel_two_grad.reshape(3, 3, chan, chan), (2, 3, 0, 1))
    return (
        pooled,
        spec_grad,
        jnp.transpose(kernel_one_grad, (2, 0, 1)),
        gain_one_grad[0],
        bias_one_grad[0],
        kernel_two_grad,
        gain_two_grad[0],
        bias_two_grad[0],
    )


def solution(mesh):
    return jax.shard_map(
        shards,
        mesh=mesh,
        in_specs=(
            P(None, "mel", "tm"),
            P(),
            P(),
            P(),
            P(),
            P(),
            P(),
            P(),
            P(None, None, "mel", "tm"),
        ),
        out_specs=(P(None, None, "mel", "tm"), P(None, "mel", "tm"), P(), P(), P(), P(), P(), P()),
        check_vma=False,
    )
```

```python
import math

import jax
import jax.numpy as jnp
from jax import lax
from jax.experimental import pallas as pl
from jax.experimental.pallas import tpu as pltpu
from jax.sharding import PartitionSpec as P

F32 = jnp.float32
BF16 = jnp.bfloat16
AXES = ("mel", "tm")
EXACT = lax.Precision.HIGHEST
RIM = 128
BAND = 24
MEL_ROWS = 16
FIRST = 24
SUMS, EDGES, COLUMNS = 16, 19, 23
SIDE = 96
SECOND = 8


def iota(shape, dim):
    return lax.broadcasted_iota(jnp.int32, shape, dim)


def dot(a, b, over=((1,), (0,)), precision=None):
    return lax.dot_general(a, b, (over, ((), ())), precision=precision, preferred_element_type=F32)


def to_column(lanes, count, start=0):
    shape = (count, lanes.shape[1])
    return jnp.sum(jnp.where(iota(shape, 1) == iota(shape, 0) + start, lanes, 0.0), axis=1, keepdims=True)


def to_lanes(column, start=0, width=128):
    shape = (column.shape[0], width)
    return jnp.sum(jnp.where(iota(shape, 1) == iota(shape, 0) + start, column, 0.0), axis=0, keepdims=True)


def halves(v):
    total = v[:, :128]
    for n in range(128, v.shape[1], 128):
        total = total + v[:, n : n + 128]
    return total


def frame_masks(bounds, frames):
    last = bounds.shape[1] - 1

    def living(f):
        return (f >= 0) & (f < bounds[0, last])

    def paired(f):
        both = living(f) & living(f + 1)
        for k in range(1, last):
            both = both & (f + 1 != bounds[0, k])
        return both

    return tuple(m.astype(F32) for m in (living(frames), paired(frames - 1), paired(frames)))


def row_valid(row, rows):
    mel = lax.axis_index("mel") * rows + row
    return ((mel >= 0) & (mel < lax.axis_size("mel") * rows)).astype(F32)


def start_all(*pairs, sems):
    copies = [pltpu.make_async_copy(src, dst, sems.at[n]) for n, (src, dst) in enumerate(pairs)]
    for copy in copies:
        copy.start()
    return copies


def wait_all(copies):
    for copy in copies:
        copy.wait()


def shifted_frames(value, behind, ahead):
    wide = value.shape[1]
    return pltpu.roll(value, 1, 1) * behind, pltpu.roll(value, wide - 1, 1) * ahead


def three_parts(v):
    high = lax.reduce_precision(v, 8, 7)
    mid = lax.reduce_precision(v - high, 8, 7)
    return high, mid, v - high - mid


def share_of(devices, chan):
    return -(-chan // devices)


def pack(spec_hbm, grad_hbm, bounds_hbm, out, own, spec, masks, bounds, edges, rows_out, sems):
    copies = start_all((bounds_hbm, bounds), (spec_hbm, spec), (grad_hbm, own), sems=sems)
    copies[0].wait()
    wide = masks.shape[1]
    frame_dev = wide - RIM
    devices = out.shape[0]
    rows = MEL_ROWS
    lane = iota((1, wide), 1)
    frames = lax.axis_index("tm") * frame_dev + jnp.where(lane < frame_dev + RIM // 2, lane, lane - wide)
    last = bounds.shape[1] - 1
    pixels = (bounds[0, last] * (lax.axis_size("mel") * rows)).astype(F32)
    found = frame_masks(bounds, frames)
    masks[...] = jnp.concatenate(
        list(found) + [jnp.full((1, wide), 1.0) * pixels, jnp.zeros((4, wide), F32)], axis=0
    )
    usable, behind, ahead = (m[:, :frame_dev] for m in found)
    copies[1].wait()
    x = spec[0].astype(F32) * usable
    lane = iota((1, frame_dev), 1)
    row = iota((rows, 1), 0)
    inner = jnp.where((lane > 0) & (lane < frame_dev - 1), usable, 0.0)
    number = (rows - 2) * jnp.sum(inner, axis=1, keepdims=True)
    inner = inner * ((row > 0) & (row < rows - 1)).astype(F32)
    centre = jnp.sum(jnp.sum(x, axis=0, keepdims=True), axis=1, keepdims=True)
    centre = centre / (rows * jnp.maximum(jnp.sum(usable, axis=1, keepdims=True), 1.0))
    centre = lax.reduce_precision(centre, 8, 7)
    shifted = [pltpu.roll(x, 1, 1) * behind, x, pltpu.roll(x, frame_dev - 1, 1) * ahead]
    taps = [pltpu.roll(v, (1 - i) % rows, 0) if i != 1 else v for i in range(3) for v in shifted]
    features = feature_rows(centre, (taps, inner))
    lane = iota((1, 128), 1)
    features = jnp.where(lane == 90, centre, jnp.where(lane == 91, number, features))
    pick = iota((8, frame_dev), 0)
    column = jnp.where(pick < 4, pick, frame_dev - 8 + pick)
    strip = dot((iota((8, frame_dev), 1) == column).astype(BF16), x.astype(BF16), ((1,), (1,)))
    lane = iota((8, 128), 1)
    repeat = (iota((rows, 128), 1) % rows == iota((rows, 128), 0)).astype(BF16)
    strip = jnp.where(lane // rows == iota((8, 128), 0), dot(strip.astype(BF16), repeat), 0.0)
    strip = jnp.sum(strip, axis=0, keepdims=True)

    def put(n, value):
        rows_out[pl.ds(n, devices, stride=FIRST), :] = jnp.broadcast_to(value, (devices, 128))

    near = jnp.concatenate([x[0:4], x[rows - 4 :]], axis=0)
    near = jnp.concatenate([near[:, :128], near[:, 128:]], axis=0)
    for d in range(devices):
        rows_out[FIRST * d : FIRST * d + 16, :] = near
    put(COLUMNS, strip)
    copies[2].wait()
    _, chan, many, half = own.shape
    share = share_of(devices, chan)
    holders = chan // share
    g = own[0].astype(F32)
    edges[0:chan] = g[:, 0, :]
    edges[chan:] = g[:, many - 1, :]

    def spread_out(v):
        if holders < devices:
            v = jnp.concatenate([v, jnp.zeros((devices - holders, 128), F32)], axis=0)
        return v

    for n in range(share):
        put(EDGES + n, spread_out(edges[n * holders : (n + 1) * holders, :]))
        put(EDGES + share + n, spread_out(edges[chan + n * holders : chan + (n + 1) * holders, :]))
    for n in range(2 * share, COLUMNS - EDGES):
        put(EDGES + n, jnp.zeros((1, 128), F32))
    end = iota((8, half), 0)
    at = iota((8, half), 1)
    ends = ((end == 0) & (at == 0)) | ((end == 1) & (at == half - 1))
    columns = dot(ends.astype(BF16), g.reshape(chan * many, half).astype(BF16), ((1,), (1,)))
    group = 128 // many
    source = iota((128, 128), 0)
    lane = iota((group, 128), 1)
    mine = lane // many == iota((group, 128), 0)
    parts = three_parts(features)
    for n in range(2):
        side = jnp.zeros((holders, 128), F32)
        for m in range(share):
            move = (iota((128, 128), 1) == SIDE + many * m + source % many).astype(BF16)
            first = m * holders * many // 128
            block = [columns[n : n + 1, 128 * q : 128 * (q + 1)] for q in range(first, first + holders * many // 128)]
            block = jnp.concatenate([jnp.where(mine, v, 0.0) for v in block], axis=0)
            side = side + dot(block.astype(BF16), move)
        put(SUMS + n, spread_out(side) + parts[n])
    put(SUMS + 2, parts[2])
    out[...] = rows_out[...].reshape(out.shape).astype(BF16)


def weights(own, bounds_hbm, k2_hbm, k1_hbm, gain_one_hbm, bias_one_hbm, gain_two_hbm, bias_two_hbm,
            wf, wb, w1, ws_hbm, pairs, singles, k1t, params, all_masks, edge_masks, twice, own_rows,
            k2, k1, vectors, bounds, ws, temp, sems):
    loads = start_all(
        (bounds_hbm, bounds),
        (k2_hbm, k2),
        (k1_hbm, k1),
        (gain_one_hbm, vectors.at[0]),
        (bias_one_hbm, vectors.at[1]),
        (gain_two_hbm, vectors.at[2]),
        (bias_two_hbm, vectors.at[3]),
        sems=sems,
    )
    _, many, count, half = own.shape
    temp[...] = own[0].astype(F32).reshape(many * count, half)
    for r in range(count):
        own_rows[r * many : (r + 1) * many] = temp[pl.ds(r, many, stride=count), :].astype(BF16)
    wait_all(loads)
    chan = k2.shape[1]
    span = wf.shape[1]
    taps = [k2[t].astype(F32) for t in range(9)]
    rest = jnp.zeros((chan, span - 9 * chan), F32)
    forward = jnp.concatenate(taps + [rest], axis=1)
    backward = jnp.concatenate([taps[8 - t].T for t in range(9)] + [rest], axis=1)
    for r in range(wb.shape[0] // chan):
        at = slice(r * chan, (r + 1) * chan)
        wb[at] = (pltpu.roll(backward, 3 * chan * r, 1) if r else backward).astype(BF16)
    full = jnp.concatenate([k1[n].astype(F32) for n in range(3)] + [jnp.zeros((7, chan), F32)], axis=0)
    low = [
        jnp.concatenate([full[3 * (2 - a) + 2 - b : 3 * (2 - a) + 3 - b] for a in range(3)], axis=1)
        for b in range(3)
    ]
    rest = jnp.zeros((1, ws.shape[1] - 3 * chan), F32)
    for b in range(3):
        base = jnp.concatenate([low[b], rest], axis=1)
        many = ws.shape[0] // 3
        rolled = [pltpu.roll(base, chan * m, 1) if m else base for m in range(many)]
        ws[many * b : many * (b + 1)] = jnp.concatenate(rolled, axis=0).astype(BF16)
    store_ws = pltpu.make_async_copy(ws, ws_hbm, sems.at[7])
    store_ws.start()
    count, frame_dev = all_masks.shape[0] // 3, all_masks.shape[1]
    frames = iota((count, frame_dev), 0) * frame_dev + iota((count, frame_dev), 1)
    for n, mask in enumerate(frame_masks(bounds, frames)):
        all_masks[n * count : (n + 1) * count] = mask
    q = iota(edge_masks.shape, 0)
    lane = iota(edge_masks.shape, 1)
    k = q % 8
    frames = (q // 8) * frame_dev + jnp.where(k < 4, k, k + frame_dev - 8)
    living, behind, ahead = frame_masks(bounds, frames)
    living = jnp.where((k == 0) | (k == 7), living, 0.0)
    edge_masks[...] = jnp.where(lane == 0, living, jnp.where(lane == 1, behind, jnp.where(lane == 2, ahead, 0.0)))
    params[...] = jnp.concatenate(
        [vectors[n] for n in range(4)] + [jnp.zeros((4, chan), F32)], axis=0
    )
    tap = iota((16, 128), 0)
    lane = iota((16, 128), 1)
    i = (tap * 11) >> 5
    ninth = (lane * 57) >> 9
    to_band = (lane == BAND * (tap - 3 * i) + i) & (tap < 9)
    to_left = (ninth == tap) & (tap < 9)
    to_right = (lane - 9 * ninth == tap) & (lane < 81)
    to_single = (lane == 81 + tap) & (tap < 9)
    source = iota((128, 128), 0) - 81
    lane = iota((128, 128), 1)
    ninth = (lane * 57) >> 9
    inside = (source >= 0) & (source < 9) & (lane < 81)
    twice[...] = jnp.where(inside, (source == ninth).astype(F32) + (source == lane - 9 * ninth).astype(F32), 0.0)
    for r in range(wf.shape[0] // chan):
        at = slice(r * chan, (r + 1) * chan)
        wf[at] = (pltpu.roll(forward, 3 * chan * r, 1) if r else forward).astype(BF16)
    k1t[...] = full
    k = full.astype(BF16)
    lanes = [dot(k, select.astype(BF16), ((0,), (0,))) for select in (to_band, to_left, to_right, to_single)]
    pairs[...] = lanes[1] * lanes[2]
    singles[...] = lanes[3]
    for m in range(w1.shape[0] // chan):
        w1[m * chan : (m + 1) * chan] = (pltpu.roll(lanes[0], m, 1) if m else lanes[0]).astype(BF16)
    store_ws.wait()


def feature_rows(centre, *parts):
    def folded(v):
        return jnp.sum(halves(v), axis=0, keepdims=True)

    rows = [jnp.zeros((1, 128), F32)] * 96
    for taps, weight in parts:
        z = [tap - centre for tap in taps]
        for s in range(9):
            left = z[s] * weight
            rows[81 + s] = rows[81 + s] + folded(left)
            for t in range(s, 9):
                rows[9 * s + t] = rows[9 * t + s] = rows[9 * s + t] + folded(left * z[t])
    return to_lanes(jnp.sum(jnp.concatenate(rows, axis=0), axis=1, keepdims=True))


def summed_blocks(ref, devices):
    block = ref.shape[0] // devices
    period = 8 // math.gcd(block, 8)
    step = period * block
    total = ref[0:step, :]
    for at in range(step, ref.shape[0], step):
        total = total + ref[at : at + step, :]
    result = total[0:block]
    for n in range(1, period):
        result = result + total[n * block : (n + 1) * block]
    return result


def moved_rows(v, step):
    if step == 0:
        return v
    count = v.shape[0]
    if abs(step) >= count:
        return jnp.zeros_like(v)
    zero = jnp.zeros((abs(step), v.shape[1]), v.dtype)
    if step > 0:
        return jnp.concatenate([zero, v[: count - step]], axis=0)
    return jnp.concatenate([v[-step:], zero], axis=0)


def silu_halves(h):
    t = jnp.tanh(h)
    one = 1.0 + t
    return h * one, one * (1.0 + h * (1.0 - t))


def forward_one(recv, spec, pairs, singles, twice, w1, wf, params, masks, all_masks, edge_masks,
                pre_two, payload, act, x3, stats, features_out, pre_one, got, strips, halo, rows_out):
    devices = recv.shape[0]
    n_mel, count = lax.axis_size("mel"), lax.axis_size("tm")
    rows = MEL_ROWS
    mels = n_mel * rows
    wide = masks.shape[1]
    frame_dev = wide - RIM
    chan = params.shape[1]
    me_m, me_t = lax.axis_index("mel"), lax.axis_index("tm")
    usable, behind, ahead = (masks[n : n + 1] for n in range(3))
    total = masks[3:4, 0:1]
    got[...] = recv[...].astype(F32).reshape(devices * FIRST, 128)

    def every(n):
        return got[pl.ds(n, devices, stride=FIRST), :]

    lane = iota((count, 128), 1)
    bands = [got[pl.ds(FIRST * k * count + COLUMNS, count, stride=FIRST), :] for k in range(n_mel)]
    for c in range(8):
        column = jnp.zeros((count, 128), F32)
        for k, band in enumerate(bands):
            part = jnp.where(lane // rows == c, band, 0.0)
            column = column + (pltpu.roll(part, rows * (k - c) % 128, 1) if k != c else part)
        strips[pl.ds(c, count, stride=8), :] = column
    at = pl.multiple_of(FIRST * (jnp.maximum(me_m - 1, 0) * count + me_t), 8)
    above = got[pl.ds(at, 16), :] * (me_m > 0).astype(F32)
    at = pl.multiple_of(FIRST * (jnp.minimum(me_m + 1, n_mel - 1) * count + me_t), 8)
    below = got[pl.ds(at, 16), :] * (me_m < n_mel - 1).astype(F32)
    above = jnp.concatenate([above[4:8], above[12:16]], axis=1)
    below = jnp.concatenate([below[0:4], below[8:12]], axis=1)
    own = spec[0].astype(F32) * usable[:, :frame_dev]
    at = pl.multiple_of(8 * jnp.minimum(me_t + 1, count - 1), 8)
    after = strips[pl.ds(at, 8), :][:, :mels] * (me_t + 1 < count).astype(F32)
    at = pl.multiple_of(8 * jnp.maximum(me_t - 1, 0), 8)
    before = strips[pl.ds(at, 8), :][:, :mels] * (me_t > 0).astype(F32)
    sides = jnp.concatenate([after[0:4], before[4:8], jnp.zeros((8, mels), F32)], axis=0).astype(BF16)
    side = iota((16, RIM), 0)
    place = iota((16, RIM), 1) == jnp.where(side < 4, side, jnp.where(side < 8, side + RIM - 8, -1))
    halo[0:8] = jnp.zeros((8, RIM), F32)
    halo[mels : mels + 8] = jnp.zeros((8, RIM), F32)
    halo[4 : mels + 4] = dot(sides, place.astype(BF16), ((0,), (0,)))
    rim = halo[pl.ds(pl.multiple_of(me_m * rows, 8), BAND), :]
    near = jnp.concatenate([jnp.concatenate([above, own, below], axis=0), rim], axis=1)
    x3[...] = jnp.concatenate(
        [
            pltpu.roll(near, 1, 1) * behind,
            near,
            pltpu.roll(near, wide - 1, 1) * ahead,
            jnp.broadcast_to(usable, (BAND, wide)),
            jnp.zeros((128 - 4 * BAND, wide), F32),
        ],
        axis=0,
    ).astype(BF16)
    pre_one[...] = dot(w1[...], x3[...])
    lane = iota((1, 128), 1)
    parts = jnp.where(lane < 92, every(SUMS) + every(SUMS + 1) + every(SUMS + 2), 0.0)
    centres, numbers = parts[:, 90:91], parts[:, 91:92]
    centre = jnp.sum(centres * numbers, axis=0, keepdims=True)
    centre = centre / jnp.maximum(jnp.sum(numbers, axis=0, keepdims=True), 1.0)
    delta = centres - centre
    features = jnp.sum(parts + delta * numbers * jnp.where(lane < 81, delta, 1.0), axis=0, keepdims=True)
    moved = jnp.sum(delta * parts, axis=0, keepdims=True)
    def edge_row(k, n):
        first = FIRST * k * count + n
        return jnp.concatenate(
            [got[pl.ds(first, count, stride=FIRST), :], got[pl.ds(first + 8, count, stride=FIRST), :]], axis=1
        )

    edge_rows = [[edge_row(k, n) for n in (0, 1, 6, 7)] for k in range(n_mel)]
    zero = jnp.zeros((count, frame_dev), F32)
    rows_of = [[], [], []]
    for k, (top, second, fore, bottom) in enumerate(edge_rows):
        for n, v in enumerate((edge_rows[k - 1][3] if k else zero, top, second)):
            rows_of[n].append(v)
        for n, v in enumerate((fore, bottom, edge_rows[k + 1][0] if k + 1 < n_mel else zero)):
            rows_of[n].append(v)
    f_usable, f_behind, f_ahead = (all_masks[n * count : (n + 1) * count, :] for n in range(3))
    lane = iota((count, frame_dev), 1)

    def frame_before(v):
        v = pltpu.roll(v, 1, 1)
        return jnp.where(lane == 0, pltpu.roll(v, 1, 0), v) * f_behind

    def frame_after(v):
        v = pltpu.roll(v, frame_dev - 1, 1)
        return jnp.where(lane == frame_dev - 1, pltpu.roll(v, count - 1, 0), v) * f_ahead

    taps = []
    for group in rows_of:
        for move in (frame_before, lambda v: v, frame_after):
            taps.append(jnp.concatenate([move(v) for v in group], axis=1))
    f_usable = jnp.concatenate([f_usable] * (2 * n_mel), axis=1)
    borders = (taps, f_usable)
    edge = strips[...]
    q_usable, q_behind, q_ahead = (edge_masks[:, n : n + 1] for n in range(3))
    lane = iota((count * 8, 128), 1)
    inside = (lane < mels) & (lane % rows != 0) & (lane % rows != rows - 1)
    shifted = [
        pltpu.roll(edge, 1, 0) * q_behind,
        edge,
        pltpu.roll(edge, count * 8 - 1, 0) * q_ahead,
    ]
    taps = [pltpu.roll(v, (1 - i) % 128, 1) if i != 1 else v for i in range(3) for v in shifted]
    features = features + feature_rows(centre, borders, (taps, jnp.where(inside, q_usable, 0.0)))
    features = jnp.where(iota((1, 128), 1) < 90, features, 0.0)
    near_mean = jnp.sum(singles[...] * features, axis=1, keepdims=True) / total
    around = jnp.sum(singles[...], axis=1, keepdims=True)
    square = jnp.sum(pairs[...] * features, axis=1, keepdims=True)
    square = (square + 2.0 * around * jnp.sum(singles[...] * moved, axis=1, keepdims=True)) / total
    inv = lax.rsqrt(square - near_mean * near_mean + 1e-05)
    mean = near_mean + centre * around
    lane = iota((chan, 128), 1)
    stats[0:chan] = jnp.where(lane == 0, mean, jnp.where(lane == 1, inv, 0.0))
    stats[chan : chan + 8] = jnp.broadcast_to(to_lanes(near_mean), (8, 128))
    stats[chan + 8 : chan + 16] = jnp.broadcast_to(to_lanes(inv), (8, 128))
    scale = 0.5 * to_column(params[0:1], chan) * inv
    shift = 0.5 * to_column(params[1:2], chan) - mean * scale
    stats[chan + 16 :] = jnp.where(lane == 0, scale, jnp.where(lane == 1, shift, 0.0))
    scale = jnp.broadcast_to(scale, (chan, wide))
    shift = jnp.broadcast_to(shift, (chan, wide))
    ext = w1.shape[0] // chan
    block, taps = wf.shape
    first = jnp.zeros((chan, 128), F32)
    second = jnp.zeros((chan, 128), F32)
    own_mask = usable[:, :frame_dev]
    low_masks = [m.astype(BF16) for m in (usable, behind, ahead)]
    for r in range(ext):
        value, _ = silu_halves(pre_one[r * chan : (r + 1) * chan, :] * scale + shift)
        if not 0 <= r - 3 < rows:
            value = value * row_valid(r - 3, rows)
        base = r * 3 * chan
        low = value.astype(BF16) * low_masks[0]
        act[base : base + chan, :], act[base + 2 * chan : base + 3 * chan, :] = shifted_frames(low, *low_masks[1:])
        act[base + chan : base + 2 * chan, :] = low
        if r < 3 or r % 2 == 0:
            continue
        g = (r - 3) // 2
        result = dot(wf[...], act[g * 3 * block : g * 3 * block + taps, :])
        pre_two[g * block : (g + 1) * block] = result
        for q in range(2):
            if 2 <= 2 * g + q < rows + 2:
                p = result[q * chan : (q + 1) * chan, :frame_dev]
                masked = p * own_mask
                first = first + halves(masked)
                second = second + halves(masked * p)
    moved = dot(jnp.broadcast_to(moved, (8, 128)), twice[...], precision=EXACT)[0:1]
    features_out[...] = jnp.concatenate(
        [features + moved, jnp.broadcast_to(centre, (1, 128)), jnp.zeros((6, 128), F32)], axis=0
    )
    share = share_of(devices, chan)

    def put(n, value):
        rows_out[pl.ds(n, devices, stride=SECOND), :] = jnp.broadcast_to(value, (devices, 128))

    for n in range(share):
        put(3 + n, moved_rows(every(EDGES + share + n), count))
        put(3 + share + n, moved_rows(every(EDGES + n), -count))
    for n in range(3 + 2 * share, SECOND - 1):
        put(n, jnp.zeros((1, 128), F32))
    lane = iota((devices, 128), 1)
    tm = iota((devices, 128), 0) % count
    lefts = jnp.where(lane >= SIDE, every(SUMS), 0.0)
    rights = jnp.where(lane >= SIDE, every(SUMS + 1), 0.0)
    beside = jnp.zeros((devices, 128), F32)
    for n, step in enumerate((0, count, -count)):
        one = jnp.where(tm > 0, moved_rows(rights, step + 1), 0.0)
        two = jnp.where(tm < count - 1, moved_rows(lefts, step - 1), 0.0)
        beside = beside + pltpu.roll(one, (32 * n - SIDE) % 128, 1) + pltpu.roll(two, (32 * n + 16 - SIDE) % 128, 1)
    put(SECOND - 1, beside)
    first = jnp.sum(first, axis=1, keepdims=True)
    second = jnp.sum(second, axis=1, keepdims=True)
    for n, part in enumerate(three_parts(to_lanes(first) + to_lanes(second, chan))):
        put(n, part)
    payload[...] = rows_out[...].reshape(payload.shape).astype(BF16)


def sum_rows(devices, taps):
    return -(-taps // devices) + 2


def backward_scaled(recv, pre_two, act, own_rows, params, masks,
                    grad, payload, pairs, stats, sides, up, right, got, beyond):
    devices = recv.shape[0]
    got[...] = recv[...].astype(F32).reshape(devices * SECOND, 128)
    chan = params.shape[1]
    half = own_rows.shape[1]
    lane = iota((half, 2 * half), 1)
    spread = jnp.where(lane >> 1 == iota((half, 2 * half), 0), 0.25, 0.0).astype(BF16)
    rows = MEL_ROWS
    wide = pre_two.shape[1]
    frame_dev = wide - RIM
    usable = masks[0:1]
    share = share_of(devices, chan)
    holders = chan // share

    def every(n):
        return got[pl.ds(n, devices, stride=SECOND), :]

    beside = every(SECOND - 1)[:holders]
    lane = iota((holders, RIM), 1)
    many = rows // 2
    up[0 : many * chan] = dot(own_rows[...], spread)
    for n in range(share):
        first = n * holders
        beyond[first : first + holders, :] = every(3 + n)[:holders]
        beyond[chan + first : chan + first + holders, :] = every(3 + share + n)[:holders]
        for r in range(many + 2):
            at = many * n + (r if r < many else 32 + many - 1 if r == many else 64)
            left, right_of = beside[:, at : at + 1], beside[:, at + 16 : at + 17]
            side = jnp.where(lane >= RIM - 2, 0.25 * left, jnp.where(lane < 2, 0.25 * right_of, 0.0))
            sides[r * chan + first : r * chan + first + holders, :] = side
    up[many * chan :] = dot(beyond[...].astype(BF16), spread)
    total = masks[3:4, 0:1]
    sums = jnp.sum(every(0) + every(1) + every(2), axis=0, keepdims=True)
    mean = to_column(sums, chan) / total
    inv = lax.rsqrt(to_column(sums, chan, chan) / total - mean * mean + 1e-05)
    lane = iota((chan, 128), 1)
    scale = 0.5 * to_column(params[2:3], chan) * inv
    shift = 0.5 * to_column(params[3:4], chan) - mean * scale
    columns = jnp.zeros((chan, 128), F32)
    for n, column in enumerate((mean, inv, scale, shift)):
        columns = jnp.where(lane == n, column, columns)
    stats[0:chan] = columns
    stats[chan : chan + 8] = jnp.broadcast_to(to_lanes(inv), (8, 128))
    shift = jnp.broadcast_to(shift, (chan, wide))
    scale = jnp.broadcast_to(scale, (chan, wide))
    mean = jnp.broadcast_to(mean, (chan, frame_dev))
    inv = jnp.broadcast_to(inv, (chan, frame_dev))
    first = jnp.zeros((chan, 128), F32)
    second = jnp.zeros((chan, 128), F32)
    own_mask = usable[:, :frame_dev]
    right[3 * chan :] = jnp.ones((16, rows * frame_dev), BF16)
    table = jnp.zeros((9 * chan, 3 * chan + 16), F32)
    for q in list(range(2, rows + 2)) + [0, 1, rows + 2, rows + 3]:
        r = q // 2
        at = slice(q * chan, (q + 1) * chan)
        m = q - 2
        mask = 0.5 * usable if 0 <= m < rows else usable * (0.5 * row_valid(m, rows))
        if q % 2 == 0:
            spot = (r - 1 if 1 <= r <= many else many + (r > 0)) * chan
            upstream = jnp.concatenate([up[spot : spot + chan, :], sides[spot : spot + chan, :]], axis=1)
        pre = pre_two[at, :]
        value, slope = silu_halves(pre * scale + shift)
        g = upstream * slope * mask
        grad[at, :] = g
        if not 0 <= m < rows:
            continue
        g = g[:, :frame_dev]
        normed = (pre[:, :frame_dev] - mean) * inv
        first = first + halves(g * normed)
        second = second + halves(g)
        value = value[:, :frame_dev] * own_mask
        both = value if m % 2 == 0 else both + value
        if m % 2:
            pairs[(r - 1) * chan : r * chan, :] = both
        lanes = slice(m * frame_dev, (m + 1) * frame_dev)
        right[0:chan, lanes] = g.astype(BF16)
        right[chan : 2 * chan, lanes] = normed.astype(BF16)
        right[2 * chan : 3 * chan, lanes] = (g - right[0:chan, lanes].astype(F32)).astype(BF16)
        if m in (5, 11, rows - 1):
            start = m - m % 6
            left = [act[(n + 2) * 3 * chan : (n + 5) * 3 * chan, :frame_dev] for n in range(start, m + 1)]
            lanes = slice(start * frame_dev, (m + 1) * frame_dev)
            table = table + dot(jnp.concatenate(left, axis=1), right[:, lanes], ((1,), (1,)))
    first = jnp.sum(first, axis=1, keepdims=True)
    second = jnp.sum(second, axis=1, keepdims=True)
    totals = to_lanes(first) + to_lanes(second, chan)
    block = payload.shape[0] // devices
    payload[pl.ds(0, devices, stride=block), :] = jnp.broadcast_to(totals, (devices, 128))
    rest = jnp.concatenate([table[:, 2 * chan :], jnp.zeros((9 * chan, chan - 16), F32)], axis=1)
    both = table[:, : 2 * chan] + jnp.where(iota(rest.shape, 1) < chan, rest, 0.0)
    single = rest[:, chan : chan + 1]
    lane = iota((devices, 128), 1)
    constants = jnp.zeros((devices, 128), F32)
    for k in range(block - 2):
        cut, ones = both[k * devices : (k + 1) * devices], single[k * devices : (k + 1) * devices]
        short = devices - cut.shape[0]
        if short:
            cut = jnp.concatenate([cut, jnp.zeros((short, 128), F32)], axis=0)
            ones = jnp.concatenate([ones, jnp.zeros((short, 1), F32)], axis=0)
        payload[pl.ds(1 + k, devices, stride=block), :] = cut
        constants = jnp.where(lane == k, ones, constants)
    payload[pl.ds(block - 1, devices, stride=block), :] = constants


def pool(totals, pairs, out, gain_out, bias_out, temp):
    gain_out[...] = totals[0:1, : gain_out.shape[1]]
    bias_out[...] = totals[0:1, gain_out.shape[1] :]
    chan, rows, half = out.shape[1:]
    to_mean = jnp.where(iota((2 * half, half), 0) >> 1 == iota((2 * half, half), 1), 0.25, 0.0)
    pooled = dot(pairs[...], to_mean, precision=EXACT)
    for r in range(rows):
        temp[pl.ds(r, chan, stride=rows), :] = pooled[r * chan : (r + 1) * chan]
    out[0] = temp[...].reshape(chan, rows, half).astype(BF16)


def backward(recv, pre_two, grad, stats_two, w1, x3, stats, params, masks, wb,
             out, own_low, payload, totals, g3, pre_one, g1):
    chan = params.shape[1]
    rows = MEL_ROWS
    wide = pre_two.shape[1]
    frame_dev = wide - RIM
    usable = masks[0:1]
    behind, ahead = (masks[n : n + 1].astype(BF16) for n in (1, 2))
    total = masks[3:4, 0:1]
    devices = payload.shape[0] // 14
    pre_one[...] = dot(w1[3 * chan : (rows + 3) * chan], x3[:, :frame_dev])

    received = summed_blocks(recv, devices)
    sums = received[0:1]
    gain_sum, bias_sum = sums[:, :chan], sums[:, chan:]
    totals[...] = jnp.broadcast_to(sums, (8, 128))
    mean, inv = stats_two[0:chan, 0:1], stats_two[0:chan, 1:2]
    factor = to_column(params[2:3], chan) * inv
    gain_part = factor * (to_column(sums, chan) / total * inv)
    bias_part = factor * (to_column(sums, chan, chan) / total) - mean * gain_part
    gain_part = jnp.broadcast_to(gain_part, (chan, wide))
    bias_part = jnp.broadcast_to(bias_part, (chan, wide))
    factor = jnp.broadcast_to(factor, (chan, wide))
    scale = jnp.broadcast_to(stats[chan + 16 :, 0:1], (chan, frame_dev))
    shift = jnp.broadcast_to(stats[chan + 16 :, 1:2], (chan, frame_dev))
    factor_one = jnp.broadcast_to(to_column(params[0:1], chan) * stats[0:chan, 1:2], (chan, frame_dev))
    own_mask = 0.5 * usable[:, :frame_dev]
    count = pre_two.shape[0] // chan
    table = jnp.zeros((chan, 128), F32)

    def tap_sums(m):
        part = g1[m * chan : (m + 4) * chan, :]
        high = lax.reduce_precision(part, 8, 7)
        low = (part - high).astype(BF16)
        taps_in = x3[:, :frame_dev]
        products = dot(high.astype(BF16), taps_in, ((1,), (1,))) + dot(low, taps_in, ((1,), (1,)))
        moved = [pltpu.roll(products[k * chan : (k + 1) * chan], 128 - (m + k + 3), 1) for k in range(4)]
        return (moved[0] + moved[1]) + (moved[2] + moved[3])

    for q in range(count):
        at = slice(q * chan, (q + 1) * chan)
        mask = usable if 0 <= q - 2 < rows else usable * row_valid(q - 2, rows)
        low = (factor * grad[at, :] - (bias_part + pre_two[at, :] * gain_part) * mask).astype(BF16)
        out[at, :] = low
        if not 1 <= q < count - 1:
            continue
        base = (q - 1) * 3 * chan
        for n, v in enumerate((low,) + shifted_frames(low, behind, ahead)):
            spot = base + (1, 0, 2)[n] * chan
            g3[spot : spot + chan, :] = v[:, :frame_dev]
        start = q - 4
        if start < 0 or start % 2:
            continue
        result = dot(wb[...], g3[start * 3 * chan : (start + 4) * 3 * chan, :])
        for n in range(2):
            m = start + n
            at = slice(m * chan, (m + 1) * chan)
            _, slope = silu_halves(pre_one[at, :] * scale + shift)
            value = result[n * chan : (n + 1) * chan] * slope * own_mask
            own_low[at, :] = (value * factor_one).astype(BF16)
            g1[at, :] = value
        if start % 4 == 2 and start > 2:
            table = table + tap_sums(start - 6)
    table = table + tap_sums(rows - 4)
    tap = iota((16, 128), 0)
    lane = iota((16, 128), 1)
    i = (tap * 11) >> 5
    select = ((lane == BAND * (tap - 3 * i) + i) & (tap < 9)) | ((lane == 3 * BAND) & (tap == 9))
    rows10 = dot(select.astype(F32), table, ((1,), (1,)), EXACT)
    share = received.shape[0] - 2
    mine = received[1 : share + 1]
    single = to_column(received[share + 1 :], share)
    factor_l = params[2:3] * stats_two[chan : chan + 1, :chan]
    mine = mine[:, :chan] - (bias_sum * single + gain_sum * mine[:, chan:]) / total
    mine = factor_l * mine
    lower = -(-share // 2)
    mine = jnp.concatenate([mine] + [jnp.zeros((2 * lower - share, chan), F32)] * (share % 2), axis=0)
    mine = jnp.concatenate([mine[:lower], mine[lower:]], axis=1)
    if lower < 9:
        mine = jnp.concatenate([mine, jnp.zeros((9 - lower, 128), F32)], axis=0)
    sums = jnp.concatenate([rows10[0:5], rows10[5:10]], axis=1)
    block = jnp.concatenate([sums, mine], axis=0)
    block = jnp.concatenate([block] * 4, axis=0)
    for d in range(0, devices, 4):
        payload[14 * d : 14 * (d + 4), :] = block


def transposed(grad, own_low, w1, wb, x3, stats, params, masks, ws_hbm, first, ws, low, g3, rim, sem):
    load = pltpu.make_async_copy(ws_hbm, ws, sem)
    load.start()
    rows = MEL_ROWS
    chan = own_low.shape[0] // rows
    wide = grad.shape[1]
    frame_dev = wide - RIM
    count = grad.shape[0] // chan
    usable = masks[0:1]
    behind, ahead = (masks[n : n + 1].astype(BF16) for n in (1, 2))
    scale = jnp.broadcast_to(stats[chan + 16 :, 0:1], (chan, wide))
    shift = jnp.broadcast_to(stats[chan + 16 :, 1:2], (chan, wide))
    factor = jnp.broadcast_to(to_column(params[0:1], chan) * stats[0:chan, 1:2], (chan, wide))
    edge = (0, 1, 2, 3, count - 4, count - 3, count - 2, count - 1)
    for q in range(count):
        value = grad[q * chan : (q + 1) * chan, :]
        for n, v in enumerate((value,) + shifted_frames(value, behind, ahead)):
            spot = (3 * q + (1, 0, 2)[n]) * chan
            rim[spot : spot + chan, :] = v[:, frame_dev:]
            if q in edge:
                spot = (3 * edge.index(q) + (1, 0, 2)[n]) * chan
                g3[spot : spot + chan, :] = v[:, :frame_dev]
    low[chan : (rows + 1) * chan, :frame_dev] = own_low[...]

    def put(m, lanes, result, pre_one):
        at = slice((m + 1) * chan, (m + 2) * chan)
        _, slope = silu_halves(pre_one * scale[:, lanes] + shift[:, lanes])
        mask = usable[:, lanes] * (0.5 * row_valid(m, rows))
        low[at, lanes] = (result * slope * mask * factor[:, lanes]).astype(BF16)

    pre_one = dot(w1[2 * chan : (rows + 4) * chan, :], x3[:, frame_dev:])
    beside = slice(frame_dev, wide)
    for start in range(0, rows + 2, 2):
        result = dot(wb[...], rim[start * 3 * chan : (start + 4) * 3 * chan, :])
        for n in range(2):
            at = slice((start + n) * chan, (start + n + 1) * chan)
            put(start + n - 1, beside, result[n * chan : (n + 1) * chan], pre_one[at])
    own = slice(0, frame_dev)
    result = dot(wb[...], g3[: 4 * 3 * chan, :])
    put(-1, own, result[:chan], dot(w1[2 * chan : 3 * chan, :], x3[:, :frame_dev]))
    result = dot(wb[...], g3[4 * 3 * chan :, :])
    put(rows, own, result[chan:], dot(w1[(rows + 3) * chan : (rows + 4) * chan, :], x3[:, :frame_dev]))
    load.wait()
    first[...] = dot(ws[...], low[...])


def finish(recv, features, stats, k1t, first, ws, w1, x3, params, masks,
           spec_hbm, kernel_one_hbm, kernel_two_hbm, gain_hbm, bias_hbm,
           spec_grad, kernel_one, kernel_two, gain_out, bias_out, sems):
    chan = params.shape[1]
    rows = MEL_ROWS
    wide = x3.shape[1]
    frame_dev = wide - RIM
    usable, behind, ahead = (masks[n : n + 1] for n in range(3))
    total = masks[3:4, 0:1]
    gain = params[0:1]
    count = recv.shape[0] // 14
    share = -(-9 * chan // count)
    lower = -(-share // 2)
    left = [recv[pl.ds(5 + p, count, stride=14), :] for p in range(lower)]
    whole = jnp.concatenate([v[:, :chan] for v in left] + [v[:, chan:] for v in left], axis=0)
    for t in range(9):
        kernel_two[t] = whole[t * chan : (t + 1) * chan].T
    stores = [pltpu.make_async_copy(kernel_two, kernel_two_hbm, sems.at[3])]
    stores[0].start()
    sums = summed_blocks(recv, count)[0:5]
    ten = jnp.concatenate([sums[:, :chan], sums[:, chan:]], axis=0)
    bias_sum = ten[9:10]
    mean_l, inv_l = stats[chan : chan + 1, :chan], stats[chan + 8 : chan + 9, :chan]
    ten = ten - features[1:2, 0:1] * bias_sum
    k = k1t[0:9]
    gain_sum = inv_l * (jnp.sum(k * ten[0:9], axis=0, keepdims=True) - mean_l * bias_sum)
    gain_out[...] = gain_sum
    bias_out[...] = bias_sum
    for n, (source, target) in enumerate(((gain_out, gain_hbm), (bias_out, bias_hbm))):
        stores.append(pltpu.make_async_copy(source, target, sems.at[n]))
        stores[-1].start()
    factor_l = gain * inv_l
    scale = factor_l * gain_sum / total * inv_l
    scale = jnp.concatenate(
        [scale * row_valid(-1, rows)] + [scale] * rows + [scale * row_valid(rows, rows)], axis=1
    )
    many = 3 * rows

    def in_parts(v, right):
        high = lax.reduce_precision(v, 8, 7)
        v = dot(jnp.concatenate([high, v - high], axis=0).astype(BF16), right)
        return v[:many] + v[many:]

    taken = in_parts(in_parts(ws[...].astype(F32) * scale, w1[2 * chan : (rows + 4) * chan, :]), x3[...])
    taps = first[...] - taken
    moved = [taps[rows * b : rows * (b + 1)] for b in range(3)]
    mean_full = mean_l + features[1:2, 0:1] * jnp.sum(k, axis=0, keepdims=True)
    constant = jnp.sum(k * (factor_l * (bias_sum - gain_sum * inv_l * mean_full) / total), axis=1, keepdims=True)
    for a in range(3):
        row = iota((rows, 1), 0) + (a - 1) + lax.axis_index("mel") * rows
        valid = ((row >= 0) & (row < lax.axis_size("mel") * rows)).astype(F32) * usable
        for b in range(3):
            t = 3 * (2 - a) + 2 - b
            moved[b] = moved[b] - constant[t : t + 1] * valid
    result = pltpu.roll(moved[0], 1, 1) * behind + moved[1] + pltpu.roll(moved[2], wide - 1, 1) * ahead
    spec_grad[0] = (result * usable)[:, :frame_dev]
    stores.append(pltpu.make_async_copy(spec_grad, spec_hbm, sems.at[2]))
    stores[-1].start()
    row = features[0:1, :]
    lane = iota((1, 128), 1)
    gram = jnp.concatenate(
        [jnp.where(lane < 9, pltpu.roll(row, 128 - 9 * t, 1) if t else row, 0.0) for t in range(9)]
        + [jnp.zeros((7, 128), F32)],
        axis=0,
    )
    single = to_column(row, 16, 81)[0:9]
    k_rows = jnp.concatenate([k1t[...], jnp.zeros((112, chan), F32)], axis=0)
    normed_taps = inv_l * (dot(gram, k_rows, precision=EXACT)[0:9] - single * mean_l)
    grad_taps = factor_l * (ten[0:9] - (bias_sum * single + gain_sum * normed_taps) / total)
    for i in range(3):
        kernel_one[i] = grad_taps[3 * i : 3 * i + 3]
    stores.append(pltpu.make_async_copy(kernel_one, kernel_one_hbm, sems.at[4]))
    stores[-1].start()
    for store in stores:
        store.wait()


def run(kernel, outs, scratch, *args, hbm=0, apart=(), flops=10**8, size=4 * 10**6):
    vmem = pl.BlockSpec(memory_space=pltpu.VMEM)
    devices = lax.axis_size("mel") * lax.axis_size("tm")
    specs = []
    args = list(args)
    for n, a in enumerate(args):
        if hbm and n >= len(args) - hbm:
            specs.append(pl.BlockSpec(memory_space=pltpu.HBM))
            args[n] = pltpu.with_memory_space_constraint(a, pltpu.HBM)
        else:
            specs.append(vmem)
            args[n] = pltpu.with_memory_space_constraint(a, pltpu.VMEM)
    return pl.pallas_call(
        kernel,
        out_shape=outs,
        in_specs=specs,
        out_specs=[pl.BlockSpec(memory_space=pltpu.HBM) if n in apart else vmem for n in range(len(outs))],
        scratch_shapes=scratch,
        compiler_params=pltpu.CompilerParams(vmem_limit_bytes=(29 + devices // 32) * 2**20),
        cost_estimate=pl.CostEstimate(flops=flops, bytes_accessed=size, transcendentals=0),
    )(*args)


def shape(dims, dtype=F32):
    return jax.ShapeDtypeStruct(dims, dtype)


def kept(dims, dtype=F32):
    return pltpu.VMEM(dims, dtype)


def far(dims, dtype=F32):
    return pltpu.HBM(dims, dtype)


def exchange(blocks, axes=AXES):
    return lax.all_to_all(blocks, axes, 0, 0, tiled=True)


def exchange_rows(rows, axes=AXES):
    return exchange(rows[:, None, :], axes)[:, 0, :]


def shards(spectrum, clip_bounds, kernel_one, gain_one, bias_one, kernel_two, gain_two, bias_two, pooled_grad):
    _, rows, frame_dev = spectrum.shape
    chan = kernel_two.shape[0]
    n_mel, n_tm = lax.axis_size("mel"), lax.axis_size("tm")
    devices = n_mel * n_tm
    half = frame_dev // 2
    wide = frame_dev + RIM
    mels = n_mel * rows

    packed, own, spec, masks = run(
        pack,
        [
            kept((devices, FIRST, 128), BF16),
            kept(pooled_grad.shape, BF16),
            kept(spectrum.shape, BF16),
            kept((8, wide)),
        ],
        [
            pltpu.SMEM(clip_bounds.shape, jnp.int32),
            pltpu.VMEM((2 * chan, half), F32),
            pltpu.VMEM((devices * FIRST, 128), F32),
            pltpu.SemaphoreType.DMA((3,)),
        ],
        spectrum,
        pooled_grad,
        clip_bounds,
        hbm=3,
    )
    recv = exchange(packed)
    ext = rows + 6
    span = 4 * 3 * chan
    wf, wb, w1, ws, pairs, singles, k1t, params, all_masks, edge_masks, twice, own_rows = run(
        weights,
        [
            kept((2 * chan, span), BF16),
            kept((2 * chan, span), BF16),
            kept((ext * chan, 128), BF16),
            far((rows * 3, (rows + 2) * chan), BF16),
            kept((chan, 128)),
            kept((chan, 128)),
            kept((16, chan)),
            kept((8, chan)),
            kept((3 * n_tm, frame_dev)),
            kept((n_tm * 8, 128)),
            kept((128, 128)),
            kept((chan * rows // 2, half), BF16),
        ],
        [
            pltpu.VMEM((9, chan, chan), BF16),
            pltpu.VMEM((3, 3, chan), BF16),
            pltpu.VMEM((4, 1, chan), F32),
            pltpu.SMEM(clip_bounds.shape, jnp.int32),
            pltpu.VMEM((rows * 3, (rows + 2) * chan), BF16),
            pltpu.VMEM((chan * rows // 2, half), F32),
            pltpu.SemaphoreType.DMA((8,)),
        ],
        own,
        clip_bounds,
        jnp.transpose(kernel_two, (2, 3, 0, 1)).reshape(9, chan, chan),
        jnp.transpose(kernel_one, (1, 2, 0)),
        gain_one[None],
        bias_one[None],
        gain_two[None],
        bias_two[None],
        hbm=7,
        apart=(3,),
    )
    pre_two, payload, act, x3, stats_one, features = run(
        forward_one,
        [
            kept(((rows + 4) * chan, wide)),
            kept((devices, SECOND, 128), BF16),
            kept((ext * 3 * chan, wide), BF16),
            kept((128, wide), BF16),
            kept((2 * chan + 16, 128)),
            kept((8, 128)),
        ],
        [
            pltpu.VMEM((ext * chan, wide), F32),
            pltpu.VMEM((devices * FIRST, 128), F32),
            pltpu.VMEM((n_tm * 8, 128), F32),
            pltpu.VMEM((mels + 8, RIM), F32),
            pltpu.VMEM((devices * SECOND, 128), F32),
        ],
        recv,
        spec,
        pairs,
        singles,
        twice,
        w1,
        wf,
        params,
        masks,
        all_masks,
        edge_masks,
    )
    recv = exchange(payload)
    grad, payload, row_pairs, stats_two = run(
        backward_scaled,
        [
            kept(((rows + 4) * chan, wide)),
            kept((devices * sum_rows(devices, 9 * chan), 128)),
            kept((rows // 2 * chan, frame_dev)),
            kept((chan + 8, 128)),
        ],
        [
            pltpu.VMEM(((rows // 2 + 2) * chan, RIM), F32),
            pltpu.VMEM(((rows // 2 + 2) * chan, frame_dev), F32),
            pltpu.VMEM((3 * chan + 16, rows * frame_dev), BF16),
            pltpu.VMEM((devices * SECOND, 128), F32),
            pltpu.VMEM((2 * chan, half), F32),
        ],
        recv,
        pre_two,
        act,
        own_rows,
        params,
        masks,
    )
    recv = exchange_rows(payload)
    grad, own_low, payload, totals = run(
        backward,
        [
            kept(((rows + 4) * chan, wide), BF16),
            kept((rows * chan, frame_dev), BF16),
            kept((devices * 14, 128)),
            kept((8, 128)),
        ],
        [
            pltpu.VMEM(((rows + 2) * 3 * chan, frame_dev), BF16),
            pltpu.VMEM((rows * chan, frame_dev), F32),
            pltpu.VMEM((rows * chan, frame_dev), F32),
        ],
        recv,
        pre_two,
        grad,
        stats_two,
        w1,
        x3,
        stats_one,
        params,
        masks,
        wb,
    )
    recv = exchange_rows(payload)
    pooled, gain_two_grad, bias_two_grad = run(
        pool,
        [shape((1, chan, rows // 2, half), BF16), shape((1, chan)), shape((1, chan))],
        [
            pltpu.VMEM((rows // 2 * chan, 128), F32),
        ],
        totals,
        row_pairs,
    )
    first, ws = run(
        transposed,
        [
            kept((rows * 3, wide)),
            kept((rows * 3, (rows + 2) * chan), BF16),
        ],
        [
            pltpu.VMEM(((rows + 2) * chan, wide), BF16),
            pltpu.VMEM((8 * 3 * chan, frame_dev), BF16),
            pltpu.VMEM(((rows + 4) * 3 * chan, RIM), BF16),
            pltpu.SemaphoreType.DMA,
        ],
        grad,
        own_low,
        w1,
        wb,
        x3,
        stats_one,
        params,
        masks,
        ws,
        hbm=1,
    )
    spec_grad, kernel_one_grad, kernel_two_grad, gain_one_grad, bias_one_grad = run(
        finish,
        [
            shape((1, rows, frame_dev)),
            shape((3, 3, chan)),
            shape((9, chan, chan)),
            shape((1, chan)),
            shape((1, chan)),
        ],
        [
            pltpu.VMEM((1, rows, frame_dev), F32),
            pltpu.VMEM((3, 3, chan), F32),
            pltpu.VMEM((9, chan, chan), F32),
            pltpu.VMEM((1, chan), F32),
            pltpu.VMEM((1, chan), F32),
            pltpu.SemaphoreType.DMA((5,)),
        ],
        recv,
        features,
        stats_one,
        k1t,
        first,
        ws,
        w1,
        x3,
        params,
        masks,
        apart=range(5),
    )
    kernel_two_grad = jnp.transpose(kernel_two_grad.reshape(3, 3, chan, chan), (2, 3, 0, 1))
    return (
        pooled,
        spec_grad,
        jnp.transpose(kernel_one_grad, (2, 0, 1)),
        gain_one_grad[0],
        bias_one_grad[0],
        kernel_two_grad,
        gain_two_grad[0],
        bias_two_grad[0],
    )


def solution(mesh):
    return jax.shard_map(
        shards,
        mesh=mesh,
        in_specs=(
            P(None, "mel", "tm"),
            P(),
            P(),
            P(),
            P(),
            P(),
            P(),
            P(),
            P(None, None, "mel", "tm"),
        ),
        out_specs=(P(None, None, "mel", "tm"), P(None, "mel", "tm"), P(), P(), P(), P(), P(), P()),
        check_vma=False,
    )
```

```python
import math

import jax
import jax.numpy as jnp
from jax import lax
from jax.experimental import pallas as pl
from jax.experimental.pallas import tpu as pltpu
from jax.sharding import PartitionSpec as P

F32 = jnp.float32
BF16 = jnp.bfloat16
AXES = ("mel", "tm")
EXACT = lax.Precision.HIGHEST
RIM = 128
BAND = 24
MEL_ROWS = 16
FIRST = 24
SUMS, EDGES, COLUMNS = 16, 19, 23
SIDE = 96
SECOND = 8


def iota(shape, dim):
    return lax.broadcasted_iota(jnp.int32, shape, dim)


def dot(a, b, over=((1,), (0,)), precision=None):
    return lax.dot_general(a, b, (over, ((), ())), precision=precision, preferred_element_type=F32)


def to_column(lanes, count, start=0):
    shape = (count, lanes.shape[1])
    return jnp.sum(jnp.where(iota(shape, 1) == iota(shape, 0) + start, lanes, 0.0), axis=1, keepdims=True)


def to_lanes(column, start=0, width=128):
    shape = (column.shape[0], width)
    return jnp.sum(jnp.where(iota(shape, 1) == iota(shape, 0) + start, column, 0.0), axis=0, keepdims=True)


def halves(v):
    total = v[:, :128]
    for n in range(128, v.shape[1], 128):
        total = total + v[:, n : n + 128]
    return total


def frame_masks(bounds, frames):
    last = bounds.shape[1] - 1

    def living(f):
        return (f >= 0) & (f < bounds[0, last])

    def paired(f):
        both = living(f) & living(f + 1)
        for k in range(1, last):
            both = both & (f + 1 != bounds[0, k])
        return both

    return tuple(m.astype(F32) for m in (living(frames), paired(frames - 1), paired(frames)))


def row_valid(row, rows):
    mel = lax.axis_index("mel") * rows + row
    return ((mel >= 0) & (mel < lax.axis_size("mel") * rows)).astype(F32)


def start_all(*pairs, sems):
    copies = [pltpu.make_async_copy(src, dst, sems.at[n]) for n, (src, dst) in enumerate(pairs)]
    for copy in copies:
        copy.start()
    return copies


def wait_all(copies):
    for copy in copies:
        copy.wait()


def shifted_frames(value, behind, ahead):
    wide = value.shape[1]
    return pltpu.roll(value, 1, 1) * behind, pltpu.roll(value, wide - 1, 1) * ahead


def three_parts(v):
    high = lax.reduce_precision(v, 8, 7)
    mid = lax.reduce_precision(v - high, 8, 7)
    return high, mid, v - high - mid


def share_of(devices, chan):
    return -(-chan // devices)


def pack(spec_hbm, grad_hbm, bounds_hbm, out, own, spec, masks, bounds, edges, rows_out, sems):
    copies = start_all((bounds_hbm, bounds), (spec_hbm, spec), (grad_hbm, own), sems=sems)
    copies[0].wait()
    wide = masks.shape[1]
    frame_dev = wide - RIM
    devices = out.shape[0]
    rows = MEL_ROWS
    lane = iota((1, wide), 1)
    frames = lax.axis_index("tm") * frame_dev + jnp.where(lane < frame_dev + RIM // 2, lane, lane - wide)
    last = bounds.shape[1] - 1
    pixels = (bounds[0, last] * (lax.axis_size("mel") * rows)).astype(F32)
    found = frame_masks(bounds, frames)
    masks[...] = jnp.concatenate(
        list(found) + [jnp.full((1, wide), 1.0) * pixels, jnp.zeros((4, wide), F32)], axis=0
    )
    usable, behind, ahead = (m[:, :frame_dev] for m in found)
    copies[1].wait()
    x = spec[0].astype(F32) * usable
    lane = iota((1, frame_dev), 1)
    row = iota((rows, 1), 0)
    inner = jnp.where((lane > 0) & (lane < frame_dev - 1), usable, 0.0)
    number = (rows - 2) * jnp.sum(inner, axis=1, keepdims=True)
    inner = inner * ((row > 0) & (row < rows - 1)).astype(F32)
    centre = jnp.sum(jnp.sum(x, axis=0, keepdims=True), axis=1, keepdims=True)
    centre = centre / (rows * jnp.maximum(jnp.sum(usable, axis=1, keepdims=True), 1.0))
    centre = lax.reduce_precision(centre, 8, 7)
    shifted = [pltpu.roll(x, 1, 1) * behind, x, pltpu.roll(x, frame_dev - 1, 1) * ahead]
    taps = [pltpu.roll(v, (1 - i) % rows, 0) if i != 1 else v for i in range(3) for v in shifted]
    features = feature_rows(centre, (taps, inner))
    lane = iota((1, 128), 1)
    features = jnp.where(lane == 90, centre, jnp.where(lane == 91, number, features))
    pick = iota((8, frame_dev), 0)
    column = jnp.where(pick < 4, pick, frame_dev - 8 + pick)
    strip = dot((iota((8, frame_dev), 1) == column).astype(BF16), x.astype(BF16), ((1,), (1,)))
    lane = iota((8, 128), 1)
    repeat = (iota((rows, 128), 1) % rows == iota((rows, 128), 0)).astype(BF16)
    strip = jnp.where(lane // rows == iota((8, 128), 0), dot(strip.astype(BF16), repeat), 0.0)
    strip = jnp.sum(strip, axis=0, keepdims=True)

    def put(n, value):
        rows_out[pl.ds(n, devices, stride=FIRST), :] = jnp.broadcast_to(value, (devices, 128))

    near = jnp.concatenate([x[0:4], x[rows - 4 :]], axis=0)
    near = jnp.concatenate([near[:, :128], near[:, 128:]], axis=0)
    for d in range(devices):
        rows_out[FIRST * d : FIRST * d + 16, :] = near
    put(COLUMNS, strip)
    copies[2].wait()
    _, chan, many, half = own.shape
    share = share_of(devices, chan)
    holders = chan // share
    g = own[0].astype(F32)
    edges[0:chan] = g[:, 0, :]
    edges[chan:] = g[:, many - 1, :]

    def spread_out(v):
        if holders < devices:
            v = jnp.concatenate([v, jnp.zeros((devices - holders, 128), F32)], axis=0)
        return v

    for n in range(share):
        put(EDGES + n, spread_out(edges[n * holders : (n + 1) * holders, :]))
        put(EDGES + share + n, spread_out(edges[chan + n * holders : chan + (n + 1) * holders, :]))
    for n in range(2 * share, COLUMNS - EDGES):
        put(EDGES + n, jnp.zeros((1, 128), F32))
    end = iota((8, half), 0)
    at = iota((8, half), 1)
    ends = ((end == 0) & (at == 0)) | ((end == 1) & (at == half - 1))
    columns = dot(ends.astype(BF16), g.reshape(chan * many, half).astype(BF16), ((1,), (1,)))
    group = 128 // many
    source = iota((128, 128), 0)
    lane = iota((group, 128), 1)
    mine = lane // many == iota((group, 128), 0)
    parts = three_parts(features)
    for n in range(2):
        side = jnp.zeros((holders, 128), F32)
        for m in range(share):
            move = (iota((128, 128), 1) == SIDE + many * m + source % many).astype(BF16)
            first = m * holders * many // 128
            block = [columns[n : n + 1, 128 * q : 128 * (q + 1)] for q in range(first, first + holders * many // 128)]
            block = jnp.concatenate([jnp.where(mine, v, 0.0) for v in block], axis=0)
            side = side + dot(block.astype(BF16), move)
        put(SUMS + n, spread_out(side) + parts[n])
    put(SUMS + 2, parts[2])
    out[...] = rows_out[...].reshape(out.shape).astype(BF16)


def weights(own, bounds_hbm, k2_hbm, k1_hbm, gain_one_hbm, bias_one_hbm, gain_two_hbm, bias_two_hbm,
            wf, wb, w1, ws_hbm, pairs, singles, k1t, params, all_masks, edge_masks, twice, own_rows,
            k2, k1, vectors, bounds, ws, temp, sems):
    loads = start_all(
        (bounds_hbm, bounds),
        (k2_hbm, k2),
        (k1_hbm, k1),
        (gain_one_hbm, vectors.at[0]),
        (bias_one_hbm, vectors.at[1]),
        (gain_two_hbm, vectors.at[2]),
        (bias_two_hbm, vectors.at[3]),
        sems=sems,
    )
    _, many, count, half = own.shape
    temp[...] = own[0].astype(F32).reshape(many * count, half)
    for r in range(count):
        own_rows[r * many : (r + 1) * many] = temp[pl.ds(r, many, stride=count), :].astype(BF16)
    wait_all(loads)
    chan = k2.shape[1]
    span = wf.shape[1]
    taps = [k2[t].astype(F32) for t in range(9)]
    rest = jnp.zeros((chan, span - 9 * chan), F32)
    forward = jnp.concatenate(taps + [rest], axis=1)
    backward = jnp.concatenate([taps[8 - t].T for t in range(9)] + [rest], axis=1)
    for r in range(wb.shape[0] // chan):
        at = slice(r * chan, (r + 1) * chan)
        wb[at] = (pltpu.roll(backward, 3 * chan * r, 1) if r else backward).astype(BF16)
    full = jnp.concatenate([k1[n].astype(F32) for n in range(3)] + [jnp.zeros((7, chan), F32)], axis=0)
    low = [
        jnp.concatenate([full[3 * (2 - a) + 2 - b : 3 * (2 - a) + 3 - b] for a in range(3)], axis=1)
        for b in range(3)
    ]
    rest = jnp.zeros((1, ws.shape[1] - 3 * chan), F32)
    for b in range(3):
        base = jnp.concatenate([low[b], rest], axis=1)
        many = ws.shape[0] // 3
        rolled = [pltpu.roll(base, chan * m, 1) if m else base for m in range(many)]
        ws[many * b : many * (b + 1)] = jnp.concatenate(rolled, axis=0).astype(BF16)
    store_ws = pltpu.make_async_copy(ws, ws_hbm, sems.at[7])
    store_ws.start()
    count, frame_dev = all_masks.shape[0] // 3, all_masks.shape[1]
    frames = iota((count, frame_dev), 0) * frame_dev + iota((count, frame_dev), 1)
    for n, mask in enumerate(frame_masks(bounds, frames)):
        all_masks[n * count : (n + 1) * count] = mask
    q = iota(edge_masks.shape, 0)
    lane = iota(edge_masks.shape, 1)
    k = q % 8
    frames = (q // 8) * frame_dev + jnp.where(k < 4, k, k + frame_dev - 8)
    living, behind, ahead = frame_masks(bounds, frames)
    living = jnp.where((k == 0) | (k == 7), living, 0.0)
    edge_masks[...] = jnp.where(lane == 0, living, jnp.where(lane == 1, behind, jnp.where(lane == 2, ahead, 0.0)))
    params[...] = jnp.concatenate(
        [vectors[n] for n in range(4)] + [jnp.zeros((4, chan), F32)], axis=0
    )
    tap = iota((16, 128), 0)
    lane = iota((16, 128), 1)
    i = (tap * 11) >> 5
    ninth = (lane * 57) >> 9
    to_band = (lane == BAND * (tap - 3 * i) + i) & (tap < 9)
    to_left = (ninth == tap) & (tap < 9)
    to_right = (lane - 9 * ninth == tap) & (lane < 81)
    to_single = (lane == 81 + tap) & (tap < 9)
    source = iota((128, 128), 0) - 81
    lane = iota((128, 128), 1)
    ninth = (lane * 57) >> 9
    inside = (source >= 0) & (source < 9) & (lane < 81)
    twice[...] = jnp.where(inside, (source == ninth).astype(F32) + (source == lane - 9 * ninth).astype(F32), 0.0)
    for r in range(wf.shape[0] // chan):
        at = slice(r * chan, (r + 1) * chan)
        wf[at] = (pltpu.roll(forward, 3 * chan * r, 1) if r else forward).astype(BF16)
    k1t[...] = full
    k = full.astype(BF16)
    lanes = [dot(k, select.astype(BF16), ((0,), (0,))) for select in (to_band, to_left, to_right, to_single)]
    pairs[...] = lanes[1] * lanes[2]
    singles[...] = lanes[3]
    for m in range(w1.shape[0] // chan):
        w1[m * chan : (m + 1) * chan] = (pltpu.roll(lanes[0], m, 1) if m else lanes[0]).astype(BF16)
    store_ws.wait()


def feature_rows(centre, *parts):
    def folded(v):
        return jnp.sum(halves(v), axis=0, keepdims=True)

    rows = [jnp.zeros((1, 128), F32)] * 96
    for taps, weight in parts:
        z = [tap - centre for tap in taps]
        for s in range(9):
            left = z[s] * weight
            rows[81 + s] = rows[81 + s] + folded(left)
            for t in range(s, 9):
                rows[9 * s + t] = rows[9 * t + s] = rows[9 * s + t] + folded(left * z[t])
    return to_lanes(jnp.sum(jnp.concatenate(rows, axis=0), axis=1, keepdims=True))


def summed_blocks(ref, devices):
    block = ref.shape[0] // devices
    period = 8 // math.gcd(block, 8)
    step = period * block
    total = ref[0:step, :]
    for at in range(step, ref.shape[0], step):
        total = total + ref[at : at + step, :]
    result = total[0:block]
    for n in range(1, period):
        result = result + total[n * block : (n + 1) * block]
    return result


def moved_rows(v, step):
    if step == 0:
        return v
    count = v.shape[0]
    if abs(step) >= count:
        return jnp.zeros_like(v)
    zero = jnp.zeros((abs(step), v.shape[1]), v.dtype)
    if step > 0:
        return jnp.concatenate([zero, v[: count - step]], axis=0)
    return jnp.concatenate([v[-step:], zero], axis=0)


def silu_halves(h):
    t = jnp.tanh(h)
    one = 1.0 + t
    return h * one, one * (1.0 + h * (1.0 - t))


def forward_one(recv, spec, pairs, singles, twice, w1, wf, params, masks, all_masks, edge_masks,
                pre_two, payload, act, x3, stats, features_out, pre_one, got, strips, halo, rows_out):
    devices = recv.shape[0]
    n_mel, count = lax.axis_size("mel"), lax.axis_size("tm")
    rows = MEL_ROWS
    mels = n_mel * rows
    wide = masks.shape[1]
    frame_dev = wide - RIM
    chan = params.shape[1]
    me_m, me_t = lax.axis_index("mel"), lax.axis_index("tm")
    usable, behind, ahead = (masks[n : n + 1] for n in range(3))
    total = masks[3:4, 0:1]
    got[...] = recv[...].astype(F32).reshape(devices * FIRST, 128)

    def every(n):
        return got[pl.ds(n, devices, stride=FIRST), :]

    lane = iota((count, 128), 1)
    bands = [got[pl.ds(FIRST * k * count + COLUMNS, count, stride=FIRST), :] for k in range(n_mel)]
    for c in range(8):
        column = jnp.zeros((count, 128), F32)
        for k, band in enumerate(bands):
            part = jnp.where(lane // rows == c, band, 0.0)
            column = column + (pltpu.roll(part, rows * (k - c) % 128, 1) if k != c else part)
        strips[pl.ds(c, count, stride=8), :] = column
    at = pl.multiple_of(FIRST * (jnp.maximum(me_m - 1, 0) * count + me_t), 8)
    above = got[pl.ds(at, 16), :] * (me_m > 0).astype(F32)
    at = pl.multiple_of(FIRST * (jnp.minimum(me_m + 1, n_mel - 1) * count + me_t), 8)
    below = got[pl.ds(at, 16), :] * (me_m < n_mel - 1).astype(F32)
    above = jnp.concatenate([above[4:8], above[12:16]], axis=1)
    below = jnp.concatenate([below[0:4], below[8:12]], axis=1)
    own = spec[0].astype(F32) * usable[:, :frame_dev]
    at = pl.multiple_of(8 * jnp.minimum(me_t + 1, count - 1), 8)
    after = strips[pl.ds(at, 8), :][:, :mels] * (me_t + 1 < count).astype(F32)
    at = pl.multiple_of(8 * jnp.maximum(me_t - 1, 0), 8)
    before = strips[pl.ds(at, 8), :][:, :mels] * (me_t > 0).astype(F32)
    sides = jnp.concatenate([after[0:4], before[4:8], jnp.zeros((8, mels), F32)], axis=0).astype(BF16)
    side = iota((16, RIM), 0)
    place = iota((16, RIM), 1) == jnp.where(side < 4, side, jnp.where(side < 8, side + RIM - 8, -1))
    halo[0:8] = jnp.zeros((8, RIM), F32)
    halo[mels : mels + 8] = jnp.zeros((8, RIM), F32)
    halo[4 : mels + 4] = dot(sides, place.astype(BF16), ((0,), (0,)))
    rim = halo[pl.ds(pl.multiple_of(me_m * rows, 8), BAND), :]
    near = jnp.concatenate([jnp.concatenate([above, own, below], axis=0), rim], axis=1)
    x3[...] = jnp.concatenate(
        [
            pltpu.roll(near, 1, 1) * behind,
            near,
            pltpu.roll(near, wide - 1, 1) * ahead,
            jnp.broadcast_to(usable, (BAND, wide)),
            jnp.zeros((128 - 4 * BAND, wide), F32),
        ],
        axis=0,
    ).astype(BF16)
    pre_one[...] = dot(w1[...], x3[...])
    lane = iota((1, 128), 1)
    parts = jnp.where(lane < 92, every(SUMS) + every(SUMS + 1) + every(SUMS + 2), 0.0)
    centres, numbers = parts[:, 90:91], parts[:, 91:92]
    centre = jnp.sum(centres * numbers, axis=0, keepdims=True)
    centre = centre / jnp.maximum(jnp.sum(numbers, axis=0, keepdims=True), 1.0)
    delta = centres - centre
    features = jnp.sum(parts + delta * numbers * jnp.where(lane < 81, delta, 1.0), axis=0, keepdims=True)
    moved = jnp.sum(delta * parts, axis=0, keepdims=True)
    def edge_row(k, n):
        first = FIRST * k * count + n
        return jnp.concatenate(
            [got[pl.ds(first, count, stride=FIRST), :], got[pl.ds(first + 8, count, stride=FIRST), :]], axis=1
        )

    edge_rows = [[edge_row(k, n) for n in (0, 1, 6, 7)] for k in range(n_mel)]
    zero = jnp.zeros((count, frame_dev), F32)
    rows_of = [[], [], []]
    for k, (top, second, fore, bottom) in enumerate(edge_rows):
        for n, v in enumerate((edge_rows[k - 1][3] if k else zero, top, second)):
            rows_of[n].append(v)
        for n, v in enumerate((fore, bottom, edge_rows[k + 1][0] if k + 1 < n_mel else zero)):
            rows_of[n].append(v)
    f_usable, f_behind, f_ahead = (all_masks[n * count : (n + 1) * count, :] for n in range(3))
    lane = iota((count, frame_dev), 1)

    def frame_before(v):
        v = pltpu.roll(v, 1, 1)
        return jnp.where(lane == 0, pltpu.roll(v, 1, 0), v) * f_behind

    def frame_after(v):
        v = pltpu.roll(v, frame_dev - 1, 1)
        return jnp.where(lane == frame_dev - 1, pltpu.roll(v, count - 1, 0), v) * f_ahead

    taps = []
    for group in rows_of:
        for move in (frame_before, lambda v: v, frame_after):
            taps.append(jnp.concatenate([move(v) for v in group], axis=1))
    f_usable = jnp.concatenate([f_usable] * (2 * n_mel), axis=1)
    borders = (taps, f_usable)
    edge = strips[...]
    q_usable, q_behind, q_ahead = (edge_masks[:, n : n + 1] for n in range(3))
    lane = iota((count * 8, 128), 1)
    inside = (lane < mels) & (lane % rows != 0) & (lane % rows != rows - 1)
    shifted = [
        pltpu.roll(edge, 1, 0) * q_behind,
        edge,
        pltpu.roll(edge, count * 8 - 1, 0) * q_ahead,
    ]
    taps = [pltpu.roll(v, (1 - i) % 128, 1) if i != 1 else v for i in range(3) for v in shifted]
    features = features + feature_rows(centre, borders, (taps, jnp.where(inside, q_usable, 0.0)))
    features = jnp.where(iota((1, 128), 1) < 90, features, 0.0)
    near_mean = jnp.sum(singles[...] * features, axis=1, keepdims=True) / total
    around = jnp.sum(singles[...], axis=1, keepdims=True)
    square = jnp.sum(pairs[...] * features, axis=1, keepdims=True)
    square = (square + 2.0 * around * jnp.sum(singles[...] * moved, axis=1, keepdims=True)) / total
    inv = lax.rsqrt(square - near_mean * near_mean + 1e-05)
    mean = near_mean + centre * around
    lane = iota((chan, 128), 1)
    stats[0:chan] = jnp.where(lane == 0, mean, jnp.where(lane == 1, inv, 0.0))
    stats[chan : chan + 8] = jnp.broadcast_to(to_lanes(near_mean), (8, 128))
    stats[chan + 8 : chan + 16] = jnp.broadcast_to(to_lanes(inv), (8, 128))
    scale = 0.5 * to_column(params[0:1], chan) * inv
    shift = 0.5 * to_column(params[1:2], chan) - mean * scale
    stats[chan + 16 :] = jnp.where(lane == 0, scale, jnp.where(lane == 1, shift, 0.0))
    scale = jnp.broadcast_to(scale, (chan, wide))
    shift = jnp.broadcast_to(shift, (chan, wide))
    ext = w1.shape[0] // chan
    block, taps = wf.shape
    first = jnp.zeros((chan, 128), F32)
    second = jnp.zeros((chan, 128), F32)
    own_mask = usable[:, :frame_dev]
    low_masks = [m.astype(BF16) for m in (usable, behind, ahead)]
    for r in range(ext):
        value, _ = silu_halves(pre_one[r * chan : (r + 1) * chan, :] * scale + shift)
        if not 0 <= r - 3 < rows:
            value = value * row_valid(r - 3, rows)
        base = r * 3 * chan
        low = value.astype(BF16) * low_masks[0]
        act[base : base + chan, :], act[base + 2 * chan : base + 3 * chan, :] = shifted_frames(low, *low_masks[1:])
        act[base + chan : base + 2 * chan, :] = low
        if r < 3 or r % 2 == 0:
            continue
        g = (r - 3) // 2
        result = dot(wf[...], act[g * 3 * block : g * 3 * block + taps, :frame_dev])
        pre_two[g * block : (g + 1) * block, :frame_dev] = result
        if g % 2:
            beside = [act[n * 3 * block : n * 3 * block + taps, frame_dev:] for n in (g - 1, g)]
            beside = dot(wf[...], jnp.concatenate(beside, axis=1))
            for n in range(2):
                pre_two[(g - 1 + n) * block : (g + n) * block, frame_dev:] = beside[:, n * RIM : (n + 1) * RIM]
        for q in range(2):
            if 2 <= 2 * g + q < rows + 2:
                p = result[q * chan : (q + 1) * chan]
                masked = p * own_mask
                first = first + halves(masked)
                second = second + halves(masked * p)
    moved = dot(jnp.broadcast_to(moved, (8, 128)), twice[...], precision=EXACT)[0:1]
    features_out[...] = jnp.concatenate(
        [features + moved, jnp.broadcast_to(centre, (1, 128)), jnp.zeros((6, 128), F32)], axis=0
    )
    share = share_of(devices, chan)

    def put(n, value):
        rows_out[pl.ds(n, devices, stride=SECOND), :] = jnp.broadcast_to(value, (devices, 128))

    for n in range(share):
        put(3 + n, moved_rows(every(EDGES + share + n), count))
        put(3 + share + n, moved_rows(every(EDGES + n), -count))
    for n in range(3 + 2 * share, SECOND - 1):
        put(n, jnp.zeros((1, 128), F32))
    lane = iota((devices, 128), 1)
    tm = iota((devices, 128), 0) % count
    lefts = jnp.where(lane >= SIDE, every(SUMS), 0.0)
    rights = jnp.where(lane >= SIDE, every(SUMS + 1), 0.0)
    beside = jnp.zeros((devices, 128), F32)
    for n, step in enumerate((0, count, -count)):
        one = jnp.where(tm > 0, moved_rows(rights, step + 1), 0.0)
        two = jnp.where(tm < count - 1, moved_rows(lefts, step - 1), 0.0)
        beside = beside + pltpu.roll(one, (32 * n - SIDE) % 128, 1) + pltpu.roll(two, (32 * n + 16 - SIDE) % 128, 1)
    put(SECOND - 1, beside)
    first = jnp.sum(first, axis=1, keepdims=True)
    second = jnp.sum(second, axis=1, keepdims=True)
    for n, part in enumerate(three_parts(to_lanes(first) + to_lanes(second, chan))):
        put(n, part)
    payload[...] = rows_out[...].reshape(payload.shape).astype(BF16)


def sum_rows(devices, taps):
    return -(-taps // devices) + 2


def backward_scaled(recv, pre_two, act, own_rows, params, masks,
                    grad, payload, pairs, stats, sides, up, right, got, beyond):
    devices = recv.shape[0]
    got[...] = recv[...].astype(F32).reshape(devices * SECOND, 128)
    chan = params.shape[1]
    half = own_rows.shape[1]
    lane = iota((half, 2 * half), 1)
    spread = jnp.where(lane >> 1 == iota((half, 2 * half), 0), 0.25, 0.0).astype(BF16)
    rows = MEL_ROWS
    wide = pre_two.shape[1]
    frame_dev = wide - RIM
    usable = masks[0:1]
    share = share_of(devices, chan)
    holders = chan // share

    def every(n):
        return got[pl.ds(n, devices, stride=SECOND), :]

    beside = every(SECOND - 1)[:holders]
    lane = iota((holders, RIM), 1)
    many = rows // 2
    up[0 : many * chan] = dot(own_rows[...], spread)
    for n in range(share):
        first = n * holders
        beyond[first : first + holders, :] = every(3 + n)[:holders]
        beyond[chan + first : chan + first + holders, :] = every(3 + share + n)[:holders]
        for r in range(many + 2):
            at = many * n + (r if r < many else 32 + many - 1 if r == many else 64)
            left, right_of = beside[:, at : at + 1], beside[:, at + 16 : at + 17]
            side = jnp.where(lane >= RIM - 2, 0.25 * left, jnp.where(lane < 2, 0.25 * right_of, 0.0))
            sides[r * chan + first : r * chan + first + holders, :] = side
    up[many * chan :] = dot(beyond[...].astype(BF16), spread)
    total = masks[3:4, 0:1]
    sums = jnp.sum(every(0) + every(1) + every(2), axis=0, keepdims=True)
    mean = to_column(sums, chan) / total
    inv = lax.rsqrt(to_column(sums, chan, chan) / total - mean * mean + 1e-05)
    lane = iota((chan, 128), 1)
    scale = 0.5 * to_column(params[2:3], chan) * inv
    shift = 0.5 * to_column(params[3:4], chan) - mean * scale
    columns = jnp.zeros((chan, 128), F32)
    for n, column in enumerate((mean, inv, scale, shift)):
        columns = jnp.where(lane == n, column, columns)
    stats[0:chan] = columns
    stats[chan : chan + 8] = jnp.broadcast_to(to_lanes(inv), (8, 128))
    shift = jnp.broadcast_to(shift, (chan, wide))
    scale = jnp.broadcast_to(scale, (chan, wide))
    mean = jnp.broadcast_to(mean, (chan, frame_dev))
    inv = jnp.broadcast_to(inv, (chan, frame_dev))
    first = jnp.zeros((chan, 128), F32)
    second = jnp.zeros((chan, 128), F32)
    own_mask = usable[:, :frame_dev]
    right[3 * chan :] = jnp.ones((16, rows * frame_dev), BF16)
    table = jnp.zeros((9 * chan, 3 * chan + 16), F32)
    for q in list(range(2, rows + 2)) + [0, 1, rows + 2, rows + 3]:
        r = q // 2
        at = slice(q * chan, (q + 1) * chan)
        m = q - 2
        mask = 0.5 * usable if 0 <= m < rows else usable * (0.5 * row_valid(m, rows))
        if q % 2 == 0:
            spot = (r - 1 if 1 <= r <= many else many + (r > 0)) * chan
            upstream = jnp.concatenate([up[spot : spot + chan, :], sides[spot : spot + chan, :]], axis=1)
        pre = pre_two[at, :]
        value, slope = silu_halves(pre * scale + shift)
        g = upstream * slope * mask
        grad[at, :] = g
        if not 0 <= m < rows:
            continue
        g = g[:, :frame_dev]
        normed = (pre[:, :frame_dev] - mean) * inv
        first = first + halves(g * normed)
        second = second + halves(g)
        value = value[:, :frame_dev] * own_mask
        both = value if m % 2 == 0 else both + value
        if m % 2:
            pairs[(r - 1) * chan : r * chan, :] = both
        lanes = slice(m * frame_dev, (m + 1) * frame_dev)
        right[0:chan, lanes] = g.astype(BF16)
        right[chan : 2 * chan, lanes] = normed.astype(BF16)
        right[2 * chan : 3 * chan, lanes] = (g - right[0:chan, lanes].astype(F32)).astype(BF16)
        if m in (5, 11, rows - 1):
            start = m - m % 6
            left = [act[(n + 2) * 3 * chan : (n + 5) * 3 * chan, :frame_dev] for n in range(start, m + 1)]
            lanes = slice(start * frame_dev, (m + 1) * frame_dev)
            table = table + dot(jnp.concatenate(left, axis=1), right[:, lanes], ((1,), (1,)))
    first = jnp.sum(first, axis=1, keepdims=True)
    second = jnp.sum(second, axis=1, keepdims=True)
    totals = to_lanes(first) + to_lanes(second, chan)
    block = payload.shape[0] // devices
    payload[pl.ds(0, devices, stride=block), :] = jnp.broadcast_to(totals, (devices, 128))
    rest = jnp.concatenate([table[:, 2 * chan :], jnp.zeros((9 * chan, chan - 16), F32)], axis=1)
    both = table[:, : 2 * chan] + jnp.where(iota(rest.shape, 1) < chan, rest, 0.0)
    single = rest[:, chan : chan + 1]
    lane = iota((devices, 128), 1)
    constants = jnp.zeros((devices, 128), F32)
    for k in range(block - 2):
        cut, ones = both[k * devices : (k + 1) * devices], single[k * devices : (k + 1) * devices]
        short = devices - cut.shape[0]
        if short:
            cut = jnp.concatenate([cut, jnp.zeros((short, 128), F32)], axis=0)
            ones = jnp.concatenate([ones, jnp.zeros((short, 1), F32)], axis=0)
        payload[pl.ds(1 + k, devices, stride=block), :] = cut
        constants = jnp.where(lane == k, ones, constants)
    payload[pl.ds(block - 1, devices, stride=block), :] = constants


def pool(totals, pairs, out, gain_out, bias_out, temp):
    gain_out[...] = totals[0:1, : gain_out.shape[1]]
    bias_out[...] = totals[0:1, gain_out.shape[1] :]
    chan, rows, half = out.shape[1:]
    to_mean = jnp.where(iota((2 * half, half), 0) >> 1 == iota((2 * half, half), 1), 0.25, 0.0)
    pooled = dot(pairs[...], to_mean, precision=EXACT)
    for r in range(rows):
        temp[pl.ds(r, chan, stride=rows), :] = pooled[r * chan : (r + 1) * chan]
    out[0] = temp[...].reshape(chan, rows, half).astype(BF16)


def backward(recv, pre_two, grad, stats_two, w1, x3, stats, params, masks, wb,
             out, own_low, payload, totals, g3, pre_one, g1):
    chan = params.shape[1]
    rows = MEL_ROWS
    wide = pre_two.shape[1]
    frame_dev = wide - RIM
    usable = masks[0:1]
    behind, ahead = (masks[n : n + 1].astype(BF16) for n in (1, 2))
    total = masks[3:4, 0:1]
    devices = payload.shape[0] // 14
    pre_one[...] = dot(w1[3 * chan : (rows + 3) * chan], x3[:, :frame_dev])

    received = summed_blocks(recv, devices)
    sums = received[0:1]
    gain_sum, bias_sum = sums[:, :chan], sums[:, chan:]
    totals[...] = jnp.broadcast_to(sums, (8, 128))
    mean, inv = stats_two[0:chan, 0:1], stats_two[0:chan, 1:2]
    factor = to_column(params[2:3], chan) * inv
    gain_part = factor * (to_column(sums, chan) / total * inv)
    bias_part = factor * (to_column(sums, chan, chan) / total) - mean * gain_part
    gain_part = jnp.broadcast_to(gain_part, (chan, wide))
    bias_part = jnp.broadcast_to(bias_part, (chan, wide))
    factor = jnp.broadcast_to(factor, (chan, wide))
    scale = jnp.broadcast_to(stats[chan + 16 :, 0:1], (chan, frame_dev))
    shift = jnp.broadcast_to(stats[chan + 16 :, 1:2], (chan, frame_dev))
    factor_one = jnp.broadcast_to(to_column(params[0:1], chan) * stats[0:chan, 1:2], (chan, frame_dev))
    own_mask = 0.5 * usable[:, :frame_dev]
    count = pre_two.shape[0] // chan
    table = jnp.zeros((chan, 128), F32)

    def tap_sums(m):
        part = g1[m * chan : (m + 4) * chan, :]
        high = lax.reduce_precision(part, 8, 7)
        low = (part - high).astype(BF16)
        taps_in = x3[:, :frame_dev]
        products = dot(high.astype(BF16), taps_in, ((1,), (1,))) + dot(low, taps_in, ((1,), (1,)))
        moved = [pltpu.roll(products[k * chan : (k + 1) * chan], 128 - (m + k + 3), 1) for k in range(4)]
        return (moved[0] + moved[1]) + (moved[2] + moved[3])

    for q in range(count):
        at = slice(q * chan, (q + 1) * chan)
        mask = usable if 0 <= q - 2 < rows else usable * row_valid(q - 2, rows)
        low = (factor * grad[at, :] - (bias_part + pre_two[at, :] * gain_part) * mask).astype(BF16)
        out[at, :] = low
        if not 1 <= q < count - 1:
            continue
        base = (q - 1) * 3 * chan
        for n, v in enumerate((low,) + shifted_frames(low, behind, ahead)):
            spot = base + (1, 0, 2)[n] * chan
            g3[spot : spot + chan, :] = v[:, :frame_dev]
        start = q - 4
        if start < 0 or start % 2:
            continue
        result = dot(wb[...], g3[start * 3 * chan : (start + 4) * 3 * chan, :])
        for n in range(2):
            m = start + n
            at = slice(m * chan, (m + 1) * chan)
            _, slope = silu_halves(pre_one[at, :] * scale + shift)
            value = result[n * chan : (n + 1) * chan] * slope * own_mask
            own_low[at, :] = (value * factor_one).astype(BF16)
            g1[at, :] = value
        if start % 4 == 2 and start > 2:
            table = table + tap_sums(start - 6)
    table = table + tap_sums(rows - 4)
    tap = iota((16, 128), 0)
    lane = iota((16, 128), 1)
    i = (tap * 11) >> 5
    select = ((lane == BAND * (tap - 3 * i) + i) & (tap < 9)) | ((lane == 3 * BAND) & (tap == 9))
    rows10 = dot(select.astype(F32), table, ((1,), (1,)), EXACT)
    share = received.shape[0] - 2
    mine = received[1 : share + 1]
    single = to_column(received[share + 1 :], share)
    factor_l = params[2:3] * stats_two[chan : chan + 1, :chan]
    mine = mine[:, :chan] - (bias_sum * single + gain_sum * mine[:, chan:]) / total
    mine = factor_l * mine
    lower = -(-share // 2)
    mine = jnp.concatenate([mine] + [jnp.zeros((2 * lower - share, chan), F32)] * (share % 2), axis=0)
    mine = jnp.concatenate([mine[:lower], mine[lower:]], axis=1)
    if lower < 9:
        mine = jnp.concatenate([mine, jnp.zeros((9 - lower, 128), F32)], axis=0)
    sums = jnp.concatenate([rows10[0:5], rows10[5:10]], axis=1)
    block = jnp.concatenate([sums, mine], axis=0)
    block = jnp.concatenate([block] * 4, axis=0)
    for d in range(0, devices, 4):
        payload[14 * d : 14 * (d + 4), :] = block


def transposed(grad, own_low, w1, wb, x3, stats, params, masks, ws_hbm, first, ws, low, g3, rim, sem):
    load = pltpu.make_async_copy(ws_hbm, ws, sem)
    load.start()
    rows = MEL_ROWS
    chan = own_low.shape[0] // rows
    wide = grad.shape[1]
    frame_dev = wide - RIM
    count = grad.shape[0] // chan
    usable = masks[0:1]
    behind, ahead = (masks[n : n + 1].astype(BF16) for n in (1, 2))
    scale = jnp.broadcast_to(stats[chan + 16 :, 0:1], (chan, wide))
    shift = jnp.broadcast_to(stats[chan + 16 :, 1:2], (chan, wide))
    factor = jnp.broadcast_to(to_column(params[0:1], chan) * stats[0:chan, 1:2], (chan, wide))
    edge = (0, 1, 2, 3, count - 4, count - 3, count - 2, count - 1)
    for q in range(count):
        value = grad[q * chan : (q + 1) * chan, :]
        for n, v in enumerate((value,) + shifted_frames(value, behind, ahead)):
            spot = (3 * q + (1, 0, 2)[n]) * chan
            rim[spot : spot + chan, :] = v[:, frame_dev:]
            if q in edge:
                spot = (3 * edge.index(q) + (1, 0, 2)[n]) * chan
                g3[spot : spot + chan, :] = v[:, :frame_dev]
    low[chan : (rows + 1) * chan, :frame_dev] = own_low[...]

    def put(m, lanes, result, pre_one):
        at = slice((m + 1) * chan, (m + 2) * chan)
        _, slope = silu_halves(pre_one * scale[:, lanes] + shift[:, lanes])
        mask = usable[:, lanes] * (0.5 * row_valid(m, rows))
        low[at, lanes] = (result * slope * mask * factor[:, lanes]).astype(BF16)

    pre_one = dot(w1[2 * chan : (rows + 4) * chan, :], x3[:, frame_dev:])
    beside = slice(frame_dev, wide)
    for start in range(0, rows + 2, 2):
        result = dot(wb[...], rim[start * 3 * chan : (start + 4) * 3 * chan, :])
        for n in range(2):
            at = slice((start + n) * chan, (start + n + 1) * chan)
            put(start + n - 1, beside, result[n * chan : (n + 1) * chan], pre_one[at])
    own = slice(0, frame_dev)
    result = dot(wb[...], g3[: 4 * 3 * chan, :])
    put(-1, own, result[:chan], dot(w1[2 * chan : 3 * chan, :], x3[:, :frame_dev]))
    result = dot(wb[...], g3[4 * 3 * chan :, :])
    put(rows, own, result[chan:], dot(w1[(rows + 3) * chan : (rows + 4) * chan, :], x3[:, :frame_dev]))
    load.wait()
    first[...] = dot(ws[...], low[...])


def finish(recv, features, stats, k1t, first, ws, w1, x3, params, masks,
           spec_hbm, kernel_one_hbm, kernel_two_hbm, gain_hbm, bias_hbm,
           spec_grad, kernel_one, kernel_two, gain_out, bias_out, sems):
    chan = params.shape[1]
    rows = MEL_ROWS
    wide = x3.shape[1]
    frame_dev = wide - RIM
    usable, behind, ahead = (masks[n : n + 1] for n in range(3))
    total = masks[3:4, 0:1]
    gain = params[0:1]
    count = recv.shape[0] // 14
    share = -(-9 * chan // count)
    lower = -(-share // 2)
    left = [recv[pl.ds(5 + p, count, stride=14), :] for p in range(lower)]
    whole = jnp.concatenate([v[:, :chan] for v in left] + [v[:, chan:] for v in left], axis=0)
    for t in range(9):
        kernel_two[t] = whole[t * chan : (t + 1) * chan].T
    stores = [pltpu.make_async_copy(kernel_two, kernel_two_hbm, sems.at[3])]
    stores[0].start()
    sums = summed_blocks(recv, count)[0:5]
    ten = jnp.concatenate([sums[:, :chan], sums[:, chan:]], axis=0)
    bias_sum = ten[9:10]
    mean_l, inv_l = stats[chan : chan + 1, :chan], stats[chan + 8 : chan + 9, :chan]
    ten = ten - features[1:2, 0:1] * bias_sum
    k = k1t[0:9]
    gain_sum = inv_l * (jnp.sum(k * ten[0:9], axis=0, keepdims=True) - mean_l * bias_sum)
    gain_out[...] = gain_sum
    bias_out[...] = bias_sum
    for n, (source, target) in enumerate(((gain_out, gain_hbm), (bias_out, bias_hbm))):
        stores.append(pltpu.make_async_copy(source, target, sems.at[n]))
        stores[-1].start()
    factor_l = gain * inv_l
    scale = factor_l * gain_sum / total * inv_l
    scale = jnp.concatenate(
        [scale * row_valid(-1, rows)] + [scale] * rows + [scale * row_valid(rows, rows)], axis=1
    )
    many = 3 * rows

    def in_parts(v, right):
        high = lax.reduce_precision(v, 8, 7)
        v = dot(jnp.concatenate([high, v - high], axis=0).astype(BF16), right)
        return v[:many] + v[many:]

    taken = in_parts(in_parts(ws[...].astype(F32) * scale, w1[2 * chan : (rows + 4) * chan, :]), x3[...])
    taps = first[...] - taken
    moved = [taps[rows * b : rows * (b + 1)] for b in range(3)]
    mean_full = mean_l + features[1:2, 0:1] * jnp.sum(k, axis=0, keepdims=True)
    constant = jnp.sum(k * (factor_l * (bias_sum - gain_sum * inv_l * mean_full) / total), axis=1, keepdims=True)
    for a in range(3):
        row = iota((rows, 1), 0) + (a - 1) + lax.axis_index("mel") * rows
        valid = ((row >= 0) & (row < lax.axis_size("mel") * rows)).astype(F32) * usable
        for b in range(3):
            t = 3 * (2 - a) + 2 - b
            moved[b] = moved[b] - constant[t : t + 1] * valid
    result = pltpu.roll(moved[0], 1, 1) * behind + moved[1] + pltpu.roll(moved[2], wide - 1, 1) * ahead
    spec_grad[0] = (result * usable)[:, :frame_dev]
    stores.append(pltpu.make_async_copy(spec_grad, spec_hbm, sems.at[2]))
    stores[-1].start()
    row = features[0:1, :]
    lane = iota((1, 128), 1)
    gram = jnp.concatenate(
        [jnp.where(lane < 9, pltpu.roll(row, 128 - 9 * t, 1) if t else row, 0.0) for t in range(9)]
        + [jnp.zeros((7, 128), F32)],
        axis=0,
    )
    single = to_column(row, 16, 81)[0:9]
    k_rows = jnp.concatenate([k1t[...], jnp.zeros((112, chan), F32)], axis=0)
    normed_taps = inv_l * (dot(gram, k_rows, precision=EXACT)[0:9] - single * mean_l)
    grad_taps = factor_l * (ten[0:9] - (bias_sum * single + gain_sum * normed_taps) / total)
    for i in range(3):
        kernel_one[i] = grad_taps[3 * i : 3 * i + 3]
    stores.append(pltpu.make_async_copy(kernel_one, kernel_one_hbm, sems.at[4]))
    stores[-1].start()
    for store in stores:
        store.wait()


def run(kernel, outs, scratch, *args, hbm=0, apart=(), flops=10**8, size=4 * 10**6):
    vmem = pl.BlockSpec(memory_space=pltpu.VMEM)
    devices = lax.axis_size("mel") * lax.axis_size("tm")
    specs = []
    args = list(args)
    for n, a in enumerate(args):
        if hbm and n >= len(args) - hbm:
            specs.append(pl.BlockSpec(memory_space=pltpu.HBM))
            args[n] = pltpu.with_memory_space_constraint(a, pltpu.HBM)
        else:
            specs.append(vmem)
            args[n] = pltpu.with_memory_space_constraint(a, pltpu.VMEM)
    return pl.pallas_call(
        kernel,
        out_shape=outs,
        in_specs=specs,
        out_specs=[pl.BlockSpec(memory_space=pltpu.HBM) if n in apart else vmem for n in range(len(outs))],
        scratch_shapes=scratch,
        compiler_params=pltpu.CompilerParams(vmem_limit_bytes=(29 + devices // 32) * 2**20),
        cost_estimate=pl.CostEstimate(flops=flops, bytes_accessed=size, transcendentals=0),
    )(*args)


def shape(dims, dtype=F32):
    return jax.ShapeDtypeStruct(dims, dtype)


def kept(dims, dtype=F32):
    return pltpu.VMEM(dims, dtype)


def far(dims, dtype=F32):
    return pltpu.HBM(dims, dtype)


def exchange(blocks, axes=AXES):
    return lax.all_to_all(blocks, axes, 0, 0, tiled=True)


def exchange_rows(rows, axes=AXES):
    return exchange(rows[:, None, :], axes)[:, 0, :]


def shards(spectrum, clip_bounds, kernel_one, gain_one, bias_one, kernel_two, gain_two, bias_two, pooled_grad):
    _, rows, frame_dev = spectrum.shape
    chan = kernel_two.shape[0]
    n_mel, n_tm = lax.axis_size("mel"), lax.axis_size("tm")
    devices = n_mel * n_tm
    half = frame_dev // 2
    wide = frame_dev + RIM
    mels = n_mel * rows

    packed, own, spec, masks = run(
        pack,
        [
            kept((devices, FIRST, 128), BF16),
            kept(pooled_grad.shape, BF16),
            kept(spectrum.shape, BF16),
            kept((8, wide)),
        ],
        [
            pltpu.SMEM(clip_bounds.shape, jnp.int32),
            pltpu.VMEM((2 * chan, half), F32),
            pltpu.VMEM((devices * FIRST, 128), F32),
            pltpu.SemaphoreType.DMA((3,)),
        ],
        spectrum,
        pooled_grad,
        clip_bounds,
        hbm=3,
    )
    recv = exchange(packed)
    ext = rows + 6
    span = 4 * 3 * chan
    wf, wb, w1, ws, pairs, singles, k1t, params, all_masks, edge_masks, twice, own_rows = run(
        weights,
        [
            kept((2 * chan, span), BF16),
            kept((2 * chan, span), BF16),
            kept((ext * chan, 128), BF16),
            far((rows * 3, (rows + 2) * chan), BF16),
            kept((chan, 128)),
            kept((chan, 128)),
            kept((16, chan)),
            kept((8, chan)),
            kept((3 * n_tm, frame_dev)),
            kept((n_tm * 8, 128)),
            kept((128, 128)),
            kept((chan * rows // 2, half), BF16),
        ],
        [
            pltpu.VMEM((9, chan, chan), BF16),
            pltpu.VMEM((3, 3, chan), BF16),
            pltpu.VMEM((4, 1, chan), F32),
            pltpu.SMEM(clip_bounds.shape, jnp.int32),
            pltpu.VMEM((rows * 3, (rows + 2) * chan), BF16),
            pltpu.VMEM((chan * rows // 2, half), F32),
            pltpu.SemaphoreType.DMA((8,)),
        ],
        own,
        clip_bounds,
        jnp.transpose(kernel_two, (2, 3, 0, 1)).reshape(9, chan, chan),
        jnp.transpose(kernel_one, (1, 2, 0)),
        gain_one[None],
        bias_one[None],
        gain_two[None],
        bias_two[None],
        hbm=7,
        apart=(3,),
    )
    pre_two, payload, act, x3, stats_one, features = run(
        forward_one,
        [
            kept(((rows + 4) * chan, wide)),
            kept((devices, SECOND, 128), BF16),
            kept((ext * 3 * chan, wide), BF16),
            kept((128, wide), BF16),
            kept((2 * chan + 16, 128)),
            kept((8, 128)),
        ],
        [
            pltpu.VMEM((ext * chan, wide), F32),
            pltpu.VMEM((devices * FIRST, 128), F32),
            pltpu.VMEM((n_tm * 8, 128), F32),
            pltpu.VMEM((mels + 8, RIM), F32),
            pltpu.VMEM((devices * SECOND, 128), F32),
        ],
        recv,
        spec,
        pairs,
        singles,
        twice,
        w1,
        wf,
        params,
        masks,
        all_masks,
        edge_masks,
    )
    recv = exchange(payload)
    grad, payload, row_pairs, stats_two = run(
        backward_scaled,
        [
            kept(((rows + 4) * chan, wide)),
            kept((devices * sum_rows(devices, 9 * chan), 128)),
            kept((rows // 2 * chan, frame_dev)),
            kept((chan + 8, 128)),
        ],
        [
            pltpu.VMEM(((rows // 2 + 2) * chan, RIM), F32),
            pltpu.VMEM(((rows // 2 + 2) * chan, frame_dev), F32),
            pltpu.VMEM((3 * chan + 16, rows * frame_dev), BF16),
            pltpu.VMEM((devices * SECOND, 128), F32),
            pltpu.VMEM((2 * chan, half), F32),
        ],
        recv,
        pre_two,
        act,
        own_rows,
        params,
        masks,
    )
    recv = exchange_rows(payload)
    grad, own_low, payload, totals = run(
        backward,
        [
            kept(((rows + 4) * chan, wide), BF16),
            kept((rows * chan, frame_dev), BF16),
            kept((devices * 14, 128)),
            kept((8, 128)),
        ],
        [
            pltpu.VMEM(((rows + 2) * 3 * chan, frame_dev), BF16),
            pltpu.VMEM((rows * chan, frame_dev), F32),
            pltpu.VMEM((rows * chan, frame_dev), F32),
        ],
        recv,
        pre_two,
        grad,
        stats_two,
        w1,
        x3,
        stats_one,
        params,
        masks,
        wb,
    )
    recv = exchange_rows(payload)
    pooled, gain_two_grad, bias_two_grad = run(
        pool,
        [shape((1, chan, rows // 2, half), BF16), shape((1, chan)), shape((1, chan))],
        [
            pltpu.VMEM((rows // 2 * chan, 128), F32),
        ],
        totals,
        row_pairs,
    )
    first, ws = run(
        transposed,
        [
            kept((rows * 3, wide)),
            kept((rows * 3, (rows + 2) * chan), BF16),
        ],
        [
            pltpu.VMEM(((rows + 2) * chan, wide), BF16),
            pltpu.VMEM((8 * 3 * chan, frame_dev), BF16),
            pltpu.VMEM(((rows + 4) * 3 * chan, RIM), BF16),
            pltpu.SemaphoreType.DMA,
        ],
        grad,
        own_low,
        w1,
        wb,
        x3,
        stats_one,
        params,
        masks,
        ws,
        hbm=1,
    )
    spec_grad, kernel_one_grad, kernel_two_grad, gain_one_grad, bias_one_grad = run(
        finish,
        [
            shape((1, rows, frame_dev)),
            shape((3, 3, chan)),
            shape((9, chan, chan)),
            shape((1, chan)),
            shape((1, chan)),
        ],
        [
            pltpu.VMEM((1, rows, frame_dev), F32),
            pltpu.VMEM((3, 3, chan), F32),
            pltpu.VMEM((9, chan, chan), F32),
            pltpu.VMEM((1, chan), F32),
            pltpu.VMEM((1, chan), F32),
            pltpu.SemaphoreType.DMA((5,)),
        ],
        recv,
        features,
        stats_one,
        k1t,
        first,
        ws,
        w1,
        x3,
        params,
        masks,
        apart=range(5),
    )
    kernel_two_grad = jnp.transpose(kernel_two_grad.reshape(3, 3, chan, chan), (2, 3, 0, 1))
    return (
        pooled,
        spec_grad,
        jnp.transpose(kernel_one_grad, (2, 0, 1)),
        gain_one_grad[0],
        bias_one_grad[0],
        kernel_two_grad,
        gain_two_grad[0],
        bias_two_grad[0],
    )


def solution(mesh):
    return jax.shard_map(
        shards,
        mesh=mesh,
        in_specs=(
            P(None, "mel", "tm"),
            P(),
            P(),
            P(),
            P(),
            P(),
            P(),
            P(),
            P(None, None, "mel", "tm"),
        ),
        out_specs=(P(None, None, "mel", "tm"), P(None, "mel", "tm"), P(), P(), P(), P(), P(), P()),
        check_vma=False,
    )
```

```python
import math

import jax
import jax.numpy as jnp
from jax import lax
from jax.experimental import pallas as pl
from jax.experimental.pallas import tpu as pltpu
from jax.sharding import PartitionSpec as P

F32 = jnp.float32
BF16 = jnp.bfloat16
AXES = ("mel", "tm")
EXACT = lax.Precision.HIGHEST
RIM = 128
BAND = 24
MEL_ROWS = 16
FIRST = 24
SUMS, EDGES, COLUMNS = 16, 19, 23
SIDE = 96
SECOND = 8


def iota(shape, dim):
    return lax.broadcasted_iota(jnp.int32, shape, dim)


def dot(a, b, over=((1,), (0,)), precision=None):
    return lax.dot_general(a, b, (over, ((), ())), precision=precision, preferred_element_type=F32)


def to_column(lanes, count, start=0):
    shape = (count, lanes.shape[1])
    return jnp.sum(jnp.where(iota(shape, 1) == iota(shape, 0) + start, lanes, 0.0), axis=1, keepdims=True)


def to_lanes(column, start=0, width=128):
    shape = (column.shape[0], width)
    return jnp.sum(jnp.where(iota(shape, 1) == iota(shape, 0) + start, column, 0.0), axis=0, keepdims=True)


def halves(v):
    total = v[:, :128]
    for n in range(128, v.shape[1], 128):
        total = total + v[:, n : n + 128]
    return total


def frame_masks(bounds, frames):
    last = bounds.shape[1] - 1

    def living(f):
        return (f >= 0) & (f < bounds[0, last])

    def paired(f):
        both = living(f) & living(f + 1)
        for k in range(1, last):
            both = both & (f + 1 != bounds[0, k])
        return both

    return tuple(m.astype(F32) for m in (living(frames), paired(frames - 1), paired(frames)))


def row_valid(row, rows):
    mel = lax.axis_index("mel") * rows + row
    return ((mel >= 0) & (mel < lax.axis_size("mel") * rows)).astype(F32)


def start_all(*pairs, sems):
    copies = [pltpu.make_async_copy(src, dst, sems.at[n]) for n, (src, dst) in enumerate(pairs)]
    for copy in copies:
        copy.start()
    return copies


def wait_all(copies):
    for copy in copies:
        copy.wait()


def shifted_frames(value, behind, ahead):
    wide = value.shape[1]
    return pltpu.roll(value, 1, 1) * behind, pltpu.roll(value, wide - 1, 1) * ahead


def three_parts(v):
    high = lax.reduce_precision(v, 8, 7)
    mid = lax.reduce_precision(v - high, 8, 7)
    return high, mid, v - high - mid


def share_of(devices, chan):
    return -(-chan // devices)


def pack(spec_hbm, grad_hbm, bounds_hbm, out, own, spec, masks, bounds, edges, rows_out, sems):
    copies = start_all((bounds_hbm, bounds), (spec_hbm, spec), (grad_hbm, own), sems=sems)
    copies[0].wait()
    wide = masks.shape[1]
    frame_dev = wide - RIM
    devices = out.shape[0]
    rows = MEL_ROWS
    lane = iota((1, wide), 1)
    frames = lax.axis_index("tm") * frame_dev + jnp.where(lane < frame_dev + RIM // 2, lane, lane - wide)
    last = bounds.shape[1] - 1
    pixels = (bounds[0, last] * (lax.axis_size("mel") * rows)).astype(F32)
    found = frame_masks(bounds, frames)
    masks[...] = jnp.concatenate(
        list(found) + [jnp.full((1, wide), 1.0) * pixels, jnp.zeros((4, wide), F32)], axis=0
    )
    usable, behind, ahead = (m[:, :frame_dev] for m in found)
    copies[1].wait()
    x = spec[0].astype(F32) * usable
    lane = iota((1, frame_dev), 1)
    row = iota((rows, 1), 0)
    inner = jnp.where((lane > 0) & (lane < frame_dev - 1), usable, 0.0)
    number = (rows - 2) * jnp.sum(inner, axis=1, keepdims=True)
    inner = inner * ((row > 0) & (row < rows - 1)).astype(F32)
    centre = jnp.sum(jnp.sum(x, axis=0, keepdims=True), axis=1, keepdims=True)
    centre = centre / (rows * jnp.maximum(jnp.sum(usable, axis=1, keepdims=True), 1.0))
    centre = lax.reduce_precision(centre, 8, 7)
    shifted = [pltpu.roll(x, 1, 1) * behind, x, pltpu.roll(x, frame_dev - 1, 1) * ahead]
    taps = [pltpu.roll(v, (1 - i) % rows, 0) if i != 1 else v for i in range(3) for v in shifted]
    features = feature_rows(centre, (taps, inner))
    lane = iota((1, 128), 1)
    features = jnp.where(lane == 90, centre, jnp.where(lane == 91, number, features))
    pick = iota((8, frame_dev), 0)
    column = jnp.where(pick < 4, pick, frame_dev - 8 + pick)
    strip = dot((iota((8, frame_dev), 1) == column).astype(BF16), x.astype(BF16), ((1,), (1,)))
    lane = iota((8, 128), 1)
    repeat = (iota((rows, 128), 1) % rows == iota((rows, 128), 0)).astype(BF16)
    strip = jnp.where(lane // rows == iota((8, 128), 0), dot(strip.astype(BF16), repeat), 0.0)
    strip = jnp.sum(strip, axis=0, keepdims=True)

    def put(n, value):
        rows_out[pl.ds(n, devices, stride=FIRST), :] = jnp.broadcast_to(value, (devices, 128))

    near = jnp.concatenate([x[0:4], x[rows - 4 :]], axis=0)
    near = jnp.concatenate([near[:, :128], near[:, 128:]], axis=0)
    for d in range(devices):
        rows_out[FIRST * d : FIRST * d + 16, :] = near
    put(COLUMNS, strip)
    copies[2].wait()
    _, chan, many, half = own.shape
    share = share_of(devices, chan)
    holders = chan // share
    g = own[0].astype(F32)
    edges[0:chan] = g[:, 0, :]
    edges[chan:] = g[:, many - 1, :]

    def spread_out(v):
        if holders < devices:
            v = jnp.concatenate([v, jnp.zeros((devices - holders, 128), F32)], axis=0)
        return v

    for n in range(share):
        put(EDGES + n, spread_out(edges[n * holders : (n + 1) * holders, :]))
        put(EDGES + share + n, spread_out(edges[chan + n * holders : chan + (n + 1) * holders, :]))
    for n in range(2 * share, COLUMNS - EDGES):
        put(EDGES + n, jnp.zeros((1, 128), F32))
    end = iota((8, half), 0)
    at = iota((8, half), 1)
    ends = ((end == 0) & (at == 0)) | ((end == 1) & (at == half - 1))
    columns = dot(ends.astype(BF16), g.reshape(chan * many, half).astype(BF16), ((1,), (1,)))
    group = 128 // many
    source = iota((128, 128), 0)
    lane = iota((group, 128), 1)
    mine = lane // many == iota((group, 128), 0)
    parts = three_parts(features)
    for n in range(2):
        side = jnp.zeros((holders, 128), F32)
        for m in range(share):
            move = (iota((128, 128), 1) == SIDE + many * m + source % many).astype(BF16)
            first = m * holders * many // 128
            block = [columns[n : n + 1, 128 * q : 128 * (q + 1)] for q in range(first, first + holders * many // 128)]
            block = jnp.concatenate([jnp.where(mine, v, 0.0) for v in block], axis=0)
            side = side + dot(block.astype(BF16), move)
        put(SUMS + n, spread_out(side) + parts[n])
    put(SUMS + 2, parts[2])
    out[...] = rows_out[...].reshape(out.shape).astype(BF16)


def weights(own, bounds_hbm, k2_hbm, k1_hbm, gain_one_hbm, bias_one_hbm, gain_two_hbm, bias_two_hbm,
            wf, wb, w1, ws_hbm, pairs, singles, k1t, params, all_masks, edge_masks, twice, own_rows,
            k2, k1, vectors, bounds, ws, temp, sems):
    loads = start_all(
        (bounds_hbm, bounds),
        (k2_hbm, k2),
        (k1_hbm, k1),
        (gain_one_hbm, vectors.at[0]),
        (bias_one_hbm, vectors.at[1]),
        (gain_two_hbm, vectors.at[2]),
        (bias_two_hbm, vectors.at[3]),
        sems=sems,
    )
    _, many, count, half = own.shape
    temp[...] = own[0].astype(F32).reshape(many * count, half)
    for r in range(count):
        own_rows[r * many : (r + 1) * many] = temp[pl.ds(r, many, stride=count), :].astype(BF16)
    wait_all(loads)
    chan = k2.shape[1]
    span = wf.shape[1]
    taps = [k2[t].astype(F32) for t in range(9)]
    rest = jnp.zeros((chan, span - 9 * chan), F32)
    forward = jnp.concatenate(taps + [rest], axis=1)
    backward = jnp.concatenate([taps[8 - t].T for t in range(9)] + [rest], axis=1)
    for r in range(wb.shape[0] // chan):
        at = slice(r * chan, (r + 1) * chan)
        wb[at] = (pltpu.roll(backward, 3 * chan * r, 1) if r else backward).astype(BF16)
    full = jnp.concatenate([k1[n].astype(F32) for n in range(3)] + [jnp.zeros((7, chan), F32)], axis=0)
    low = [
        jnp.concatenate([full[3 * (2 - a) + 2 - b : 3 * (2 - a) + 3 - b] for a in range(3)], axis=1)
        for b in range(3)
    ]
    rest = jnp.zeros((1, ws.shape[1] - 3 * chan), F32)
    for b in range(3):
        base = jnp.concatenate([low[b], rest], axis=1)
        many = ws.shape[0] // 3
        rolled = [pltpu.roll(base, chan * m, 1) if m else base for m in range(many)]
        ws[many * b : many * (b + 1)] = jnp.concatenate(rolled, axis=0).astype(BF16)
    store_ws = pltpu.make_async_copy(ws, ws_hbm, sems.at[7])
    store_ws.start()
    count, frame_dev = all_masks.shape[0] // 3, all_masks.shape[1]
    frames = iota((count, frame_dev), 0) * frame_dev + iota((count, frame_dev), 1)
    for n, mask in enumerate(frame_masks(bounds, frames)):
        all_masks[n * count : (n + 1) * count] = mask
    q = iota(edge_masks.shape, 0)
    lane = iota(edge_masks.shape, 1)
    k = q % 8
    frames = (q // 8) * frame_dev + jnp.where(k < 4, k, k + frame_dev - 8)
    living, behind, ahead = frame_masks(bounds, frames)
    living = jnp.where((k == 0) | (k == 7), living, 0.0)
    edge_masks[...] = jnp.where(lane == 0, living, jnp.where(lane == 1, behind, jnp.where(lane == 2, ahead, 0.0)))
    params[...] = jnp.concatenate(
        [vectors[n] for n in range(4)] + [jnp.zeros((4, chan), F32)], axis=0
    )
    tap = iota((16, 128), 0)
    lane = iota((16, 128), 1)
    i = (tap * 11) >> 5
    ninth = (lane * 57) >> 9
    to_band = (lane == BAND * (tap - 3 * i) + i) & (tap < 9)
    to_left = (ninth == tap) & (tap < 9)
    to_right = (lane - 9 * ninth == tap) & (lane < 81)
    to_single = (lane == 81 + tap) & (tap < 9)
    source = iota((128, 128), 0) - 81
    lane = iota((128, 128), 1)
    ninth = (lane * 57) >> 9
    inside = (source >= 0) & (source < 9) & (lane < 81)
    twice[...] = jnp.where(inside, (source == ninth).astype(F32) + (source == lane - 9 * ninth).astype(F32), 0.0)
    for r in range(wf.shape[0] // chan):
        at = slice(r * chan, (r + 1) * chan)
        wf[at] = (pltpu.roll(forward, 3 * chan * r, 1) if r else forward).astype(BF16)
    k1t[...] = full
    k = full.astype(BF16)
    lanes = [dot(k, select.astype(BF16), ((0,), (0,))) for select in (to_band, to_left, to_right, to_single)]
    pairs[...] = lanes[1] * lanes[2]
    singles[...] = lanes[3]
    for m in range(w1.shape[0] // chan):
        w1[m * chan : (m + 1) * chan] = (pltpu.roll(lanes[0], m, 1) if m else lanes[0]).astype(BF16)
    store_ws.wait()


def feature_rows(centre, *parts):
    def folded(v):
        return jnp.sum(halves(v), axis=0, keepdims=True)

    rows = [jnp.zeros((1, 128), F32)] * 96
    for taps, weight in parts:
        z = [tap - centre for tap in taps]
        for s in range(9):
            left = z[s] * weight
            rows[81 + s] = rows[81 + s] + folded(left)
            for t in range(s, 9):
                rows[9 * s + t] = rows[9 * t + s] = rows[9 * s + t] + folded(left * z[t])
    return to_lanes(jnp.sum(jnp.concatenate(rows, axis=0), axis=1, keepdims=True))


def summed_blocks(ref, devices):
    block = ref.shape[0] // devices
    period = 8 // math.gcd(block, 8)
    step = period * block
    total = ref[0:step, :]
    for at in range(step, ref.shape[0], step):
        total = total + ref[at : at + step, :]
    result = total[0:block]
    for n in range(1, period):
        result = result + total[n * block : (n + 1) * block]
    return result


def moved_rows(v, step):
    if step == 0:
        return v
    count = v.shape[0]
    if abs(step) >= count:
        return jnp.zeros_like(v)
    zero = jnp.zeros((abs(step), v.shape[1]), v.dtype)
    if step > 0:
        return jnp.concatenate([zero, v[: count - step]], axis=0)
    return jnp.concatenate([v[-step:], zero], axis=0)


def silu_halves(h):
    t = jnp.tanh(h)
    one = 1.0 + t
    return h * one, one * (1.0 + h * (1.0 - t))


def forward_one(recv, spec, pairs, singles, twice, w1, wf, params, masks, all_masks, edge_masks,
                pre_two, payload, act, x3, stats, features_out, pre_one, got, strips, halo, rows_out):
    devices = recv.shape[0]
    n_mel, count = lax.axis_size("mel"), lax.axis_size("tm")
    rows = MEL_ROWS
    mels = n_mel * rows
    wide = masks.shape[1]
    frame_dev = wide - RIM
    chan = params.shape[1]
    me_m, me_t = lax.axis_index("mel"), lax.axis_index("tm")
    usable, behind, ahead = (masks[n : n + 1] for n in range(3))
    total = masks[3:4, 0:1]
    got[...] = recv[...].astype(F32).reshape(devices * FIRST, 128)

    def every(n):
        return got[pl.ds(n, devices, stride=FIRST), :]

    lane = iota((count, 128), 1)
    bands = [got[pl.ds(FIRST * k * count + COLUMNS, count, stride=FIRST), :] for k in range(n_mel)]
    for c in range(8):
        column = jnp.zeros((count, 128), F32)
        for k, band in enumerate(bands):
            part = jnp.where(lane // rows == c, band, 0.0)
            column = column + (pltpu.roll(part, rows * (k - c) % 128, 1) if k != c else part)
        strips[pl.ds(c, count, stride=8), :] = column
    at = pl.multiple_of(FIRST * (jnp.maximum(me_m - 1, 0) * count + me_t), 8)
    above = got[pl.ds(at, 16), :] * (me_m > 0).astype(F32)
    at = pl.multiple_of(FIRST * (jnp.minimum(me_m + 1, n_mel - 1) * count + me_t), 8)
    below = got[pl.ds(at, 16), :] * (me_m < n_mel - 1).astype(F32)
    above = jnp.concatenate([above[4:8], above[12:16]], axis=1)
    below = jnp.concatenate([below[0:4], below[8:12]], axis=1)
    own = spec[0].astype(F32) * usable[:, :frame_dev]
    at = pl.multiple_of(8 * jnp.minimum(me_t + 1, count - 1), 8)
    after = strips[pl.ds(at, 8), :][:, :mels] * (me_t + 1 < count).astype(F32)
    at = pl.multiple_of(8 * jnp.maximum(me_t - 1, 0), 8)
    before = strips[pl.ds(at, 8), :][:, :mels] * (me_t > 0).astype(F32)
    sides = jnp.concatenate([after[0:4], before[4:8], jnp.zeros((8, mels), F32)], axis=0).astype(BF16)
    side = iota((16, RIM), 0)
    place = iota((16, RIM), 1) == jnp.where(side < 4, side, jnp.where(side < 8, side + RIM - 8, -1))
    halo[0:8] = jnp.zeros((8, RIM), F32)
    halo[mels : mels + 8] = jnp.zeros((8, RIM), F32)
    halo[4 : mels + 4] = dot(sides, place.astype(BF16), ((0,), (0,)))
    rim = halo[pl.ds(pl.multiple_of(me_m * rows, 8), BAND), :]
    near = jnp.concatenate([jnp.concatenate([above, own, below], axis=0), rim], axis=1)
    x3[...] = jnp.concatenate(
        [
            pltpu.roll(near, 1, 1) * behind,
            near,
            pltpu.roll(near, wide - 1, 1) * ahead,
            jnp.broadcast_to(usable, (BAND, wide)),
            jnp.zeros((128 - 4 * BAND, wide), F32),
        ],
        axis=0,
    ).astype(BF16)
    pre_one[...] = dot(w1[...], x3[...])
    lane = iota((1, 128), 1)
    parts = jnp.where(lane < 92, every(SUMS) + every(SUMS + 1) + every(SUMS + 2), 0.0)
    centres, numbers = parts[:, 90:91], parts[:, 91:92]
    centre = jnp.sum(centres * numbers, axis=0, keepdims=True)
    centre = centre / jnp.maximum(jnp.sum(numbers, axis=0, keepdims=True), 1.0)
    delta = centres - centre
    features = jnp.sum(parts + delta * numbers * jnp.where(lane < 81, delta, 1.0), axis=0, keepdims=True)
    moved = jnp.sum(delta * parts, axis=0, keepdims=True)
    def edge_row(k, n):
        first = FIRST * k * count + n
        return jnp.concatenate(
            [got[pl.ds(first, count, stride=FIRST), :], got[pl.ds(first + 8, count, stride=FIRST), :]], axis=1
        )

    edge_rows = [[edge_row(k, n) for n in (0, 1, 6, 7)] for k in range(n_mel)]
    zero = jnp.zeros((count, frame_dev), F32)
    rows_of = [[], [], []]
    for k, (top, second, fore, bottom) in enumerate(edge_rows):
        for n, v in enumerate((edge_rows[k - 1][3] if k else zero, top, second)):
            rows_of[n].append(v)
        for n, v in enumerate((fore, bottom, edge_rows[k + 1][0] if k + 1 < n_mel else zero)):
            rows_of[n].append(v)
    f_usable, f_behind, f_ahead = (all_masks[n * count : (n + 1) * count, :] for n in range(3))
    lane = iota((count, frame_dev), 1)

    def frame_before(v):
        v = pltpu.roll(v, 1, 1)
        return jnp.where(lane == 0, pltpu.roll(v, 1, 0), v) * f_behind

    def frame_after(v):
        v = pltpu.roll(v, frame_dev - 1, 1)
        return jnp.where(lane == frame_dev - 1, pltpu.roll(v, count - 1, 0), v) * f_ahead

    taps = []
    for group in rows_of:
        for move in (frame_before, lambda v: v, frame_after):
            taps.append(jnp.concatenate([move(v) for v in group], axis=1))
    f_usable = jnp.concatenate([f_usable] * (2 * n_mel), axis=1)
    borders = (taps, f_usable)
    edge = strips[...]
    q_usable, q_behind, q_ahead = (edge_masks[:, n : n + 1] for n in range(3))
    lane = iota((count * 8, 128), 1)
    inside = (lane < mels) & (lane % rows != 0) & (lane % rows != rows - 1)
    shifted = [
        pltpu.roll(edge, 1, 0) * q_behind,
        edge,
        pltpu.roll(edge, count * 8 - 1, 0) * q_ahead,
    ]
    taps = [pltpu.roll(v, (1 - i) % 128, 1) if i != 1 else v for i in range(3) for v in shifted]
    features = features + feature_rows(centre, borders, (taps, jnp.where(inside, q_usable, 0.0)))
    features = jnp.where(iota((1, 128), 1) < 90, features, 0.0)
    near_mean = jnp.sum(singles[...] * features, axis=1, keepdims=True) / total
    around = jnp.sum(singles[...], axis=1, keepdims=True)
    square = jnp.sum(pairs[...] * features, axis=1, keepdims=True)
    square = (square + 2.0 * around * jnp.sum(singles[...] * moved, axis=1, keepdims=True)) / total
    inv = lax.rsqrt(square - near_mean * near_mean + 1e-05)
    mean = near_mean + centre * around
    lane = iota((chan, 128), 1)
    stats[0:chan] = jnp.where(lane == 0, mean, jnp.where(lane == 1, inv, 0.0))
    stats[chan : chan + 8] = jnp.broadcast_to(to_lanes(near_mean), (8, 128))
    stats[chan + 8 : chan + 16] = jnp.broadcast_to(to_lanes(inv), (8, 128))
    scale = 0.5 * to_column(params[0:1], chan) * inv
    shift = 0.5 * to_column(params[1:2], chan) - mean * scale
    stats[chan + 16 :] = jnp.where(lane == 0, scale, jnp.where(lane == 1, shift, 0.0))
    scale = jnp.broadcast_to(scale, (chan, wide))
    shift = jnp.broadcast_to(shift, (chan, wide))
    ext = w1.shape[0] // chan
    block, taps = wf.shape
    first = jnp.zeros((chan, 128), F32)
    second = jnp.zeros((chan, 128), F32)
    own_mask = usable[:, :frame_dev]
    low_masks = [m.astype(BF16) for m in (usable, behind, ahead)]
    for r in range(ext):
        value, _ = silu_halves(pre_one[r * chan : (r + 1) * chan, :] * scale + shift)
        if not 0 <= r - 3 < rows:
            value = value * row_valid(r - 3, rows)
        base = r * 3 * chan
        low = value.astype(BF16) * low_masks[0]
        act[base : base + chan, :], act[base + 2 * chan : base + 3 * chan, :] = shifted_frames(low, *low_masks[1:])
        act[base + chan : base + 2 * chan, :] = low
        if r < 3 or r % 2 == 0:
            continue
        g = (r - 3) // 2
        result = dot(wf[...], act[g * 3 * block : g * 3 * block + taps, :frame_dev])
        pre_two[g * block : (g + 1) * block, :frame_dev] = result
        if g % 2:
            beside = [act[n * 3 * block : n * 3 * block + taps, frame_dev:] for n in (g - 1, g)]
            beside = dot(wf[...], jnp.concatenate(beside, axis=1))
            for n in range(2):
                pre_two[(g - 1 + n) * block : (g + n) * block, frame_dev:] = beside[:, n * RIM : (n + 1) * RIM]
        for q in range(2):
            if 2 <= 2 * g + q < rows + 2:
                p = result[q * chan : (q + 1) * chan]
                masked = p * own_mask
                first = first + halves(masked)
                second = second + halves(masked * p)
    moved = dot(jnp.broadcast_to(moved, (8, 128)), twice[...], precision=EXACT)[0:1]
    features_out[...] = jnp.concatenate(
        [features + moved, jnp.broadcast_to(centre, (1, 128)), jnp.zeros((6, 128), F32)], axis=0
    )
    share = share_of(devices, chan)

    def put(n, value):
        rows_out[pl.ds(n, devices, stride=SECOND), :] = jnp.broadcast_to(value, (devices, 128))

    for n in range(share):
        put(3 + n, moved_rows(every(EDGES + share + n), count))
        put(3 + share + n, moved_rows(every(EDGES + n), -count))
    for n in range(3 + 2 * share, SECOND - 1):
        put(n, jnp.zeros((1, 128), F32))
    lane = iota((devices, 128), 1)
    tm = iota((devices, 128), 0) % count
    lefts = jnp.where(lane >= SIDE, every(SUMS), 0.0)
    rights = jnp.where(lane >= SIDE, every(SUMS + 1), 0.0)
    beside = jnp.zeros((devices, 128), F32)
    for n, step in enumerate((0, count, -count)):
        one = jnp.where(tm > 0, moved_rows(rights, step + 1), 0.0)
        two = jnp.where(tm < count - 1, moved_rows(lefts, step - 1), 0.0)
        beside = beside + pltpu.roll(one, (32 * n - SIDE) % 128, 1) + pltpu.roll(two, (32 * n + 16 - SIDE) % 128, 1)
    put(SECOND - 1, beside)
    first = jnp.sum(first, axis=1, keepdims=True)
    second = jnp.sum(second, axis=1, keepdims=True)
    for n, part in enumerate(three_parts(to_lanes(first) + to_lanes(second, chan))):
        put(n, part)
    payload[...] = rows_out[...].reshape(payload.shape).astype(BF16)


def sum_rows(devices, taps):
    return -(-taps // devices) + 2


def backward_scaled(recv, pre_two, act, own_rows, params, masks,
                    grad, payload, pairs, stats, sides, up, right, got, beyond):
    devices = recv.shape[0]
    got[...] = recv[...].astype(F32).reshape(devices * SECOND, 128)
    chan = params.shape[1]
    half = own_rows.shape[1]
    lane = iota((half, 2 * half), 1)
    spread = jnp.where(lane >> 1 == iota((half, 2 * half), 0), 0.25, 0.0).astype(BF16)
    rows = MEL_ROWS
    wide = pre_two.shape[1]
    frame_dev = wide - RIM
    usable = masks[0:1]
    share = share_of(devices, chan)
    holders = chan // share

    def every(n):
        return got[pl.ds(n, devices, stride=SECOND), :]

    beside = every(SECOND - 1)[:holders]
    lane = iota((holders, RIM), 1)
    many = rows // 2
    up[0 : many * chan] = dot(own_rows[...], spread)
    for n in range(share):
        first = n * holders
        beyond[first : first + holders, :] = every(3 + n)[:holders]
        beyond[chan + first : chan + first + holders, :] = every(3 + share + n)[:holders]
        for r in range(many + 2):
            at = many * n + (r if r < many else 32 + many - 1 if r == many else 64)
            left, right_of = beside[:, at : at + 1], beside[:, at + 16 : at + 17]
            side = jnp.where(lane >= RIM - 2, 0.25 * left, jnp.where(lane < 2, 0.25 * right_of, 0.0))
            sides[r * chan + first : r * chan + first + holders, :] = side
    up[many * chan :] = dot(beyond[...].astype(BF16), spread)
    total = masks[3:4, 0:1]
    sums = jnp.sum(every(0) + every(1) + every(2), axis=0, keepdims=True)
    mean = to_column(sums, chan) / total
    inv = lax.rsqrt(to_column(sums, chan, chan) / total - mean * mean + 1e-05)
    lane = iota((chan, 128), 1)
    scale = 0.5 * to_column(params[2:3], chan) * inv
    shift = 0.5 * to_column(params[3:4], chan) - mean * scale
    columns = jnp.zeros((chan, 128), F32)
    for n, column in enumerate((mean, inv, scale, shift)):
        columns = jnp.where(lane == n, column, columns)
    stats[0:chan] = columns
    stats[chan : chan + 8] = jnp.broadcast_to(to_lanes(inv), (8, 128))
    shift = jnp.broadcast_to(shift, (chan, wide))
    scale = jnp.broadcast_to(scale, (chan, wide))
    mean = jnp.broadcast_to(mean, (chan, frame_dev))
    inv = jnp.broadcast_to(inv, (chan, frame_dev))
    first = jnp.zeros((chan, 128), F32)
    second = jnp.zeros((chan, 128), F32)
    own_mask = usable[:, :frame_dev]
    right[3 * chan :] = jnp.ones((16, rows * frame_dev), BF16)
    table = jnp.zeros((9 * chan, 3 * chan + 16), F32)
    for q in list(range(2, rows + 2)) + [0, 1, rows + 2, rows + 3]:
        r = q // 2
        at = slice(q * chan, (q + 1) * chan)
        m = q - 2
        mask = 0.5 * usable if 0 <= m < rows else usable * (0.5 * row_valid(m, rows))
        if q % 2 == 0:
            spot = (r - 1 if 1 <= r <= many else many + (r > 0)) * chan
            upstream = jnp.concatenate([up[spot : spot + chan, :], sides[spot : spot + chan, :]], axis=1)
        pre = pre_two[at, :]
        value, slope = silu_halves(pre * scale + shift)
        g = upstream * slope * mask
        grad[at, :] = g
        if not 0 <= m < rows:
            continue
        g = g[:, :frame_dev]
        normed = (pre[:, :frame_dev] - mean) * inv
        first = first + halves(g * normed)
        second = second + halves(g)
        value = value[:, :frame_dev] * own_mask
        both = value if m % 2 == 0 else both + value
        if m % 2:
            pairs[(r - 1) * chan : r * chan, :] = both
        lanes = slice(m * frame_dev, (m + 1) * frame_dev)
        right[0:chan, lanes] = g.astype(BF16)
        right[chan : 2 * chan, lanes] = normed.astype(BF16)
        right[2 * chan : 3 * chan, lanes] = (g - right[0:chan, lanes].astype(F32)).astype(BF16)
        if m in (5, 11, rows - 1):
            start = m - m % 6
            left = [act[(n + 2) * 3 * chan : (n + 5) * 3 * chan, :frame_dev] for n in range(start, m + 1)]
            lanes = slice(start * frame_dev, (m + 1) * frame_dev)
            table = table + dot(jnp.concatenate(left, axis=1), right[:, lanes], ((1,), (1,)))
    first = jnp.sum(first, axis=1, keepdims=True)
    second = jnp.sum(second, axis=1, keepdims=True)
    totals = to_lanes(first) + to_lanes(second, chan)
    block = payload.shape[0] // devices
    payload[pl.ds(0, devices, stride=block), :] = jnp.broadcast_to(totals, (devices, 128))
    rest = jnp.concatenate([table[:, 2 * chan :], jnp.zeros((9 * chan, chan - 16), F32)], axis=1)
    both = table[:, : 2 * chan] + jnp.where(iota(rest.shape, 1) < chan, rest, 0.0)
    single = rest[:, chan : chan + 1]
    lane = iota((devices, 128), 1)
    constants = jnp.zeros((devices, 128), F32)
    for k in range(block - 2):
        cut, ones = both[k * devices : (k + 1) * devices], single[k * devices : (k + 1) * devices]
        short = devices - cut.shape[0]
        if short:
            cut = jnp.concatenate([cut, jnp.zeros((short, 128), F32)], axis=0)
            ones = jnp.concatenate([ones, jnp.zeros((short, 1), F32)], axis=0)
        payload[pl.ds(1 + k, devices, stride=block), :] = cut
        constants = jnp.where(lane == k, ones, constants)
    payload[pl.ds(block - 1, devices, stride=block), :] = constants


def pool(totals, pairs, out, gain_out, bias_out, temp):
    gain_out[...] = totals[0:1, : gain_out.shape[1]]
    bias_out[...] = totals[0:1, gain_out.shape[1] :]
    chan, rows, half = out.shape[1:]
    to_mean = jnp.where(iota((2 * half, half), 0) >> 1 == iota((2 * half, half), 1), 0.25, 0.0)
    pooled = dot(pairs[...], to_mean, precision=EXACT)
    for r in range(rows):
        temp[pl.ds(r, chan, stride=rows), :] = pooled[r * chan : (r + 1) * chan]
    out[0] = temp[...].reshape(chan, rows, half).astype(BF16)


def backward(recv, pre_two, grad, stats_two, w1, x3, stats, params, masks, wb,
             out, own_low, payload, totals, g3, pre_one, g1):
    chan = params.shape[1]
    rows = MEL_ROWS
    wide = pre_two.shape[1]
    frame_dev = wide - RIM
    usable = masks[0:1]
    behind, ahead = (masks[n : n + 1].astype(BF16) for n in (1, 2))
    total = masks[3:4, 0:1]
    devices = payload.shape[0] // 14
    pre_one[...] = dot(w1[3 * chan : (rows + 3) * chan], x3[:, :frame_dev])

    received = summed_blocks(recv, devices)
    sums = received[0:1]
    gain_sum, bias_sum = sums[:, :chan], sums[:, chan:]
    totals[...] = jnp.broadcast_to(sums, (8, 128))
    mean, inv = stats_two[0:chan, 0:1], stats_two[0:chan, 1:2]
    factor = to_column(params[2:3], chan) * inv
    gain_part = factor * (to_column(sums, chan) / total * inv)
    bias_part = factor * (to_column(sums, chan, chan) / total) - mean * gain_part
    gain_part = jnp.broadcast_to(gain_part, (chan, wide))
    bias_part = jnp.broadcast_to(bias_part, (chan, wide))
    factor = jnp.broadcast_to(factor, (chan, wide))
    scale = jnp.broadcast_to(stats[chan + 16 :, 0:1], (chan, frame_dev))
    shift = jnp.broadcast_to(stats[chan + 16 :, 1:2], (chan, frame_dev))
    factor_one = jnp.broadcast_to(to_column(params[0:1], chan) * stats[0:chan, 1:2], (chan, frame_dev))
    own_mask = 0.5 * usable[:, :frame_dev]
    count = pre_two.shape[0] // chan
    table = jnp.zeros((chan, 128), F32)

    def tap_sums(m):
        part = g1[m * chan : (m + 4) * chan, :]
        high = lax.reduce_precision(part, 8, 7)
        low = (part - high).astype(BF16)
        taps_in = x3[:, :frame_dev]
        products = dot(high.astype(BF16), taps_in, ((1,), (1,))) + dot(low, taps_in, ((1,), (1,)))
        moved = [pltpu.roll(products[k * chan : (k + 1) * chan], 128 - (m + k + 3), 1) for k in range(4)]
        return (moved[0] + moved[1]) + (moved[2] + moved[3])

    for q in range(count):
        at = slice(q * chan, (q + 1) * chan)
        mask = usable if 0 <= q - 2 < rows else usable * row_valid(q - 2, rows)
        low = (factor * grad[at, :] - (bias_part + pre_two[at, :] * gain_part) * mask).astype(BF16)
        out[at, :] = low
        if not 1 <= q < count - 1:
            continue
        base = (q - 1) * 3 * chan
        for n, v in enumerate((low,) + shifted_frames(low, behind, ahead)):
            spot = base + (1, 0, 2)[n] * chan
            g3[spot : spot + chan, :] = v[:, :frame_dev]
        start = q - 4
        if start < 0 or start % 2:
            continue
        result = dot(wb[...], g3[start * 3 * chan : (start + 4) * 3 * chan, :])
        for n in range(2):
            m = start + n
            at = slice(m * chan, (m + 1) * chan)
            _, slope = silu_halves(pre_one[at, :] * scale + shift)
            value = result[n * chan : (n + 1) * chan] * slope * own_mask
            own_low[at, :] = (value * factor_one).astype(BF16)
            g1[at, :] = value
        if start % 4 == 2 and start > 2:
            table = table + tap_sums(start - 6)
    table = table + tap_sums(rows - 4)
    table = table.T
    places = [BAND * j + i for i in range(3) for j in range(3)] + [3 * BAND]
    rows10 = jnp.concatenate([table[n : n + 1] for n in places], axis=0)
    share = received.shape[0] - 2
    mine = received[1 : share + 1]
    single = to_column(received[share + 1 :], share)
    factor_l = params[2:3] * stats_two[chan : chan + 1, :chan]
    mine = mine[:, :chan] - (bias_sum * single + gain_sum * mine[:, chan:]) / total
    mine = factor_l * mine
    lower = -(-share // 2)
    mine = jnp.concatenate([mine] + [jnp.zeros((2 * lower - share, chan), F32)] * (share % 2), axis=0)
    mine = jnp.concatenate([mine[:lower], mine[lower:]], axis=1)
    if lower < 9:
        mine = jnp.concatenate([mine, jnp.zeros((9 - lower, 128), F32)], axis=0)
    sums = jnp.concatenate([rows10[0:5], rows10[5:10]], axis=1)
    block = jnp.concatenate([sums, mine], axis=0)
    block = jnp.concatenate([block] * 4, axis=0)
    for d in range(0, devices, 4):
        payload[14 * d : 14 * (d + 4), :] = block


def transposed(grad, own_low, w1, wb, x3, stats, features, k1t, params, masks, ws_hbm,
               first, ws, normed_taps, low, g3, rim, sem):
    load = pltpu.make_async_copy(ws_hbm, ws, sem)
    load.start()
    rows = MEL_ROWS
    chan = own_low.shape[0] // rows
    wide = grad.shape[1]
    frame_dev = wide - RIM
    count = grad.shape[0] // chan
    usable = masks[0:1]
    behind, ahead = (masks[n : n + 1].astype(BF16) for n in (1, 2))
    scale = jnp.broadcast_to(stats[chan + 16 :, 0:1], (chan, wide))
    shift = jnp.broadcast_to(stats[chan + 16 :, 1:2], (chan, wide))
    factor = jnp.broadcast_to(to_column(params[0:1], chan) * stats[0:chan, 1:2], (chan, wide))
    edge = (0, 1, 2, 3, count - 4, count - 3, count - 2, count - 1)
    for q in range(count):
        value = grad[q * chan : (q + 1) * chan, :]
        for n, v in enumerate((value,) + shifted_frames(value, behind, ahead)):
            spot = (3 * q + (1, 0, 2)[n]) * chan
            rim[spot : spot + chan, :] = v[:, frame_dev:]
            if q in edge:
                spot = (3 * edge.index(q) + (1, 0, 2)[n]) * chan
                g3[spot : spot + chan, :] = v[:, :frame_dev]
    low[chan : (rows + 1) * chan, :frame_dev] = own_low[...]

    def put(m, lanes, result, pre_one):
        at = slice((m + 1) * chan, (m + 2) * chan)
        _, slope = silu_halves(pre_one * scale[:, lanes] + shift[:, lanes])
        mask = usable[:, lanes] * (0.5 * row_valid(m, rows))
        low[at, lanes] = (result * slope * mask * factor[:, lanes]).astype(BF16)

    pre_one = dot(w1[2 * chan : (rows + 4) * chan, :], x3[:, frame_dev:])
    beside = slice(frame_dev, wide)
    for start in range(0, rows + 2, 2):
        result = dot(wb[...], rim[start * 3 * chan : (start + 4) * 3 * chan, :])
        for n in range(2):
            at = slice((start + n) * chan, (start + n + 1) * chan)
            put(start + n - 1, beside, result[n * chan : (n + 1) * chan], pre_one[at])
    own = slice(0, frame_dev)
    result = dot(wb[...], g3[: 4 * 3 * chan, :])
    put(-1, own, result[:chan], dot(w1[2 * chan : 3 * chan, :], x3[:, :frame_dev]))
    result = dot(wb[...], g3[4 * 3 * chan :, :])
    put(rows, own, result[chan:], dot(w1[(rows + 3) * chan : (rows + 4) * chan, :], x3[:, :frame_dev]))
    row = features[0:1, :]
    lane = iota((1, 128), 1)
    gram = jnp.concatenate(
        [jnp.where(lane < 9, pltpu.roll(row, 128 - 9 * t, 1) if t else row, 0.0) for t in range(9)]
        + [jnp.zeros((7, 128), F32)],
        axis=0,
    )
    single = to_column(row, 16, 81)[0:9]
    k_rows = jnp.concatenate([k1t[...], jnp.zeros((112, chan), F32)], axis=0)
    mean_l, inv_l = stats[chan : chan + 1, :chan], stats[chan + 8 : chan + 9, :chan]
    normed = inv_l * (dot(gram, k_rows, precision=EXACT)[0:9] - single * mean_l)
    normed_taps[0:16] = jnp.concatenate([normed, jnp.zeros((7, chan), F32)], axis=0)
    normed_taps[16:32] = jnp.broadcast_to(to_column(row, 16, 81), (16, chan))
    load.wait()
    first[...] = dot(ws[...], low[...])


def finish(recv, features, stats, k1t, first, ws, w1, x3, normed_taps, params, masks,
           spec_hbm, kernel_one_hbm, kernel_two_hbm, gain_hbm, bias_hbm,
           spec_grad, kernel_one, kernel_two, gain_out, bias_out, sems):
    chan = params.shape[1]
    rows = MEL_ROWS
    wide = x3.shape[1]
    frame_dev = wide - RIM
    usable, behind, ahead = (masks[n : n + 1] for n in range(3))
    total = masks[3:4, 0:1]
    gain = params[0:1]
    count = recv.shape[0] // 14
    share = -(-9 * chan // count)
    lower = -(-share // 2)
    left = [recv[pl.ds(5 + p, count, stride=14), :] for p in range(lower)]
    whole = jnp.concatenate([v[:, :chan] for v in left] + [v[:, chan:] for v in left], axis=0)
    for t in range(9):
        kernel_two[t] = whole[t * chan : (t + 1) * chan].T
    stores = [pltpu.make_async_copy(kernel_two, kernel_two_hbm, sems.at[4])]
    stores[0].start()
    sums = summed_blocks(recv, count)[0:5]
    ten = jnp.concatenate([sums[:, :chan], sums[:, chan:]], axis=0)
    bias_sum = ten[9:10]
    mean_l, inv_l = stats[chan : chan + 1, :chan], stats[chan + 8 : chan + 9, :chan]
    ten = ten - features[1:2, 0:1] * bias_sum
    k = k1t[0:9]
    gain_sum = inv_l * (jnp.sum(k * ten[0:9], axis=0, keepdims=True) - mean_l * bias_sum)
    gain_out[...] = gain_sum
    bias_out[...] = bias_sum
    factor_l = gain * inv_l
    scale = factor_l * gain_sum / total * inv_l
    scale = jnp.concatenate(
        [scale * row_valid(-1, rows)] + [scale] * rows + [scale * row_valid(rows, rows)], axis=1
    )
    many = 3 * rows

    def in_parts(v, right):
        high = lax.reduce_precision(v, 8, 7)
        v = dot(jnp.concatenate([high, v - high], axis=0).astype(BF16), right)
        return v[:many] + v[many:]

    taken = in_parts(in_parts(ws[...].astype(F32) * scale, w1[2 * chan : (rows + 4) * chan, :]), x3[...])
    taps = first[...] - taken
    moved = [taps[rows * b : rows * (b + 1)] for b in range(3)]
    mean_full = mean_l + features[1:2, 0:1] * jnp.sum(k, axis=0, keepdims=True)
    constant = jnp.sum(k * (factor_l * (bias_sum - gain_sum * inv_l * mean_full) / total), axis=1, keepdims=True)
    for a in range(3):
        row = iota((rows, 1), 0) + (a - 1) + lax.axis_index("mel") * rows
        valid = ((row >= 0) & (row < lax.axis_size("mel") * rows)).astype(F32) * usable
        for b in range(3):
            t = 3 * (2 - a) + 2 - b
            moved[b] = moved[b] - constant[t : t + 1] * valid
    result = pltpu.roll(moved[0], 1, 1) * behind + moved[1] + pltpu.roll(moved[2], wide - 1, 1) * ahead
    spec_grad[0] = (result * usable)[:, :frame_dev]
    grad_taps = factor_l * (ten[0:9] - (bias_sum * normed_taps[16:25] + gain_sum * normed_taps[0:9]) / total)
    for i in range(3):
        kernel_one[i] = grad_taps[3 * i : 3 * i + 3]
    outs = ((spec_grad, spec_hbm), (kernel_one, kernel_one_hbm), (gain_out, gain_hbm), (bias_out, bias_hbm))
    wait_all(stores + start_all(*outs, sems=sems))


def run(kernel, outs, scratch, *args, hbm=0, apart=(), flops=10**8, size=4 * 10**6):
    vmem = pl.BlockSpec(memory_space=pltpu.VMEM)
    devices = lax.axis_size("mel") * lax.axis_size("tm")
    specs = []
    args = list(args)
    for n, a in enumerate(args):
        if hbm and n >= len(args) - hbm:
            specs.append(pl.BlockSpec(memory_space=pltpu.HBM))
            args[n] = pltpu.with_memory_space_constraint(a, pltpu.HBM)
        else:
            specs.append(vmem)
            args[n] = pltpu.with_memory_space_constraint(a, pltpu.VMEM)
    return pl.pallas_call(
        kernel,
        out_shape=outs,
        in_specs=specs,
        out_specs=[pl.BlockSpec(memory_space=pltpu.HBM) if n in apart else vmem for n in range(len(outs))],
        scratch_shapes=scratch,
        compiler_params=pltpu.CompilerParams(vmem_limit_bytes=(29 + devices // 32) * 2**20),
        cost_estimate=pl.CostEstimate(flops=flops, bytes_accessed=size, transcendentals=0),
    )(*args)


def shape(dims, dtype=F32):
    return jax.ShapeDtypeStruct(dims, dtype)


def kept(dims, dtype=F32):
    return pltpu.VMEM(dims, dtype)


def far(dims, dtype=F32):
    return pltpu.HBM(dims, dtype)


def exchange(blocks, axes=AXES):
    return lax.all_to_all(blocks, axes, 0, 0, tiled=True)


def exchange_rows(rows, axes=AXES):
    return exchange(rows[:, None, :], axes)[:, 0, :]


def shards(spectrum, clip_bounds, kernel_one, gain_one, bias_one, kernel_two, gain_two, bias_two, pooled_grad):
    _, rows, frame_dev = spectrum.shape
    chan = kernel_two.shape[0]
    n_mel, n_tm = lax.axis_size("mel"), lax.axis_size("tm")
    devices = n_mel * n_tm
    half = frame_dev // 2
    wide = frame_dev + RIM
    mels = n_mel * rows

    packed, own, spec, masks = run(
        pack,
        [
            kept((devices, FIRST, 128), BF16),
            kept(pooled_grad.shape, BF16),
            kept(spectrum.shape, BF16),
            kept((8, wide)),
        ],
        [
            pltpu.SMEM(clip_bounds.shape, jnp.int32),
            pltpu.VMEM((2 * chan, half), F32),
            pltpu.VMEM((devices * FIRST, 128), F32),
            pltpu.SemaphoreType.DMA((3,)),
        ],
        spectrum,
        pooled_grad,
        clip_bounds,
        hbm=3,
    )
    recv = exchange(packed)
    ext = rows + 6
    span = 4 * 3 * chan
    wf, wb, w1, ws, pairs, singles, k1t, params, all_masks, edge_masks, twice, own_rows = run(
        weights,
        [
            kept((2 * chan, span), BF16),
            kept((2 * chan, span), BF16),
            kept((ext * chan, 128), BF16),
            far((rows * 3, (rows + 2) * chan), BF16),
            kept((chan, 128)),
            kept((chan, 128)),
            kept((16, chan)),
            kept((8, chan)),
            kept((3 * n_tm, frame_dev)),
            kept((n_tm * 8, 128)),
            kept((128, 128)),
            kept((chan * rows // 2, half), BF16),
        ],
        [
            pltpu.VMEM((9, chan, chan), BF16),
            pltpu.VMEM((3, 3, chan), BF16),
            pltpu.VMEM((4, 1, chan), F32),
            pltpu.SMEM(clip_bounds.shape, jnp.int32),
            pltpu.VMEM((rows * 3, (rows + 2) * chan), BF16),
            pltpu.VMEM((chan * rows // 2, half), F32),
            pltpu.SemaphoreType.DMA((8,)),
        ],
        own,
        clip_bounds,
        jnp.transpose(kernel_two, (2, 3, 0, 1)).reshape(9, chan, chan),
        jnp.transpose(kernel_one, (1, 2, 0)),
        gain_one[None],
        bias_one[None],
        gain_two[None],
        bias_two[None],
        hbm=7,
        apart=(3,),
    )
    pre_two, payload, act, x3, stats_one, features = run(
        forward_one,
        [
            kept(((rows + 4) * chan, wide)),
            kept((devices, SECOND, 128), BF16),
            kept((ext * 3 * chan, wide), BF16),
            kept((128, wide), BF16),
            kept((2 * chan + 16, 128)),
            kept((8, 128)),
        ],
        [
            pltpu.VMEM((ext * chan, wide), F32),
            pltpu.VMEM((devices * FIRST, 128), F32),
            pltpu.VMEM((n_tm * 8, 128), F32),
            pltpu.VMEM((mels + 8, RIM), F32),
            pltpu.VMEM((devices * SECOND, 128), F32),
        ],
        recv,
        spec,
        pairs,
        singles,
        twice,
        w1,
        wf,
        params,
        masks,
        all_masks,
        edge_masks,
    )
    recv = exchange(payload)
    grad, payload, row_pairs, stats_two = run(
        backward_scaled,
        [
            kept(((rows + 4) * chan, wide)),
            kept((devices * sum_rows(devices, 9 * chan), 128)),
            kept((rows // 2 * chan, frame_dev)),
            kept((chan + 8, 128)),
        ],
        [
            pltpu.VMEM(((rows // 2 + 2) * chan, RIM), F32),
            pltpu.VMEM(((rows // 2 + 2) * chan, frame_dev), F32),
            pltpu.VMEM((3 * chan + 16, rows * frame_dev), BF16),
            pltpu.VMEM((devices * SECOND, 128), F32),
            pltpu.VMEM((2 * chan, half), F32),
        ],
        recv,
        pre_two,
        act,
        own_rows,
        params,
        masks,
    )
    recv = exchange_rows(payload)
    grad, own_low, payload, totals = run(
        backward,
        [
            kept(((rows + 4) * chan, wide), BF16),
            kept((rows * chan, frame_dev), BF16),
            kept((devices * 14, 128)),
            kept((8, 128)),
        ],
        [
            pltpu.VMEM(((rows + 2) * 3 * chan, frame_dev), BF16),
            pltpu.VMEM((rows * chan, frame_dev), F32),
            pltpu.VMEM((rows * chan, frame_dev), F32),
        ],
        recv,
        pre_two,
        grad,
        stats_two,
        w1,
        x3,
        stats_one,
        params,
        masks,
        wb,
    )
    recv = exchange_rows(payload)
    pooled, gain_two_grad, bias_two_grad = run(
        pool,
        [shape((1, chan, rows // 2, half), BF16), shape((1, chan)), shape((1, chan))],
        [
            pltpu.VMEM((rows // 2 * chan, 128), F32),
        ],
        totals,
        row_pairs,
    )
    first, ws, normed_taps = run(
        transposed,
        [
            kept((rows * 3, wide)),
            kept((rows * 3, (rows + 2) * chan), BF16),
            kept((32, chan)),
        ],
        [
            pltpu.VMEM(((rows + 2) * chan, wide), BF16),
            pltpu.VMEM((8 * 3 * chan, frame_dev), BF16),
            pltpu.VMEM(((rows + 4) * 3 * chan, RIM), BF16),
            pltpu.SemaphoreType.DMA,
        ],
        grad,
        own_low,
        w1,
        wb,
        x3,
        stats_one,
        features,
        k1t,
        params,
        masks,
        ws,
        hbm=1,
    )
    spec_grad, kernel_one_grad, kernel_two_grad, gain_one_grad, bias_one_grad = run(
        finish,
        [
            shape((1, rows, frame_dev)),
            shape((3, 3, chan)),
            shape((9, chan, chan)),
            shape((1, chan)),
            shape((1, chan)),
        ],
        [
            pltpu.VMEM((1, rows, frame_dev), F32),
            pltpu.VMEM((3, 3, chan), F32),
            pltpu.VMEM((9, chan, chan), F32),
            pltpu.VMEM((1, chan), F32),
            pltpu.VMEM((1, chan), F32),
            pltpu.SemaphoreType.DMA((5,)),
        ],
        recv,
        features,
        stats_one,
        k1t,
        first,
        ws,
        w1,
        x3,
        normed_taps,
        params,
        masks,
        apart=range(5),
    )
    kernel_two_grad = jnp.transpose(kernel_two_grad.reshape(3, 3, chan, chan), (2, 3, 0, 1))
    return (
        pooled,
        spec_grad,
        jnp.transpose(kernel_one_grad, (2, 0, 1)),
        gain_one_grad[0],
        bias_one_grad[0],
        kernel_two_grad,
        gain_two_grad[0],
        bias_two_grad[0],
    )


def solution(mesh):
    return jax.shard_map(
        shards,
        mesh=mesh,
        in_specs=(
            P(None, "mel", "tm"),
            P(),
            P(),
            P(),
            P(),
            P(),
            P(),
            P(),
            P(None, None, "mel", "tm"),
        ),
        out_specs=(P(None, None, "mel", "tm"), P(None, "mel", "tm"), P(), P(), P(), P(), P(), P()),
        check_vma=False,
    )
```

```python
import math

import jax
import jax.numpy as jnp
from jax import lax
from jax.experimental import pallas as pl
from jax.experimental.pallas import tpu as pltpu
from jax.sharding import PartitionSpec as P

F32 = jnp.float32
BF16 = jnp.bfloat16
AXES = ("mel", "tm")
EXACT = lax.Precision.HIGHEST
RIM = 128
BAND = 24
MEL_ROWS = 16
FIRST = 24
SUMS, EDGES, COLUMNS = 16, 19, 23
SIDE = 96
SECOND = 8


def iota(shape, dim):
    return lax.broadcasted_iota(jnp.int32, shape, dim)


def dot(a, b, over=((1,), (0,)), precision=None):
    return lax.dot_general(a, b, (over, ((), ())), precision=precision, preferred_element_type=F32)


def to_column(lanes, count, start=0):
    shape = (count, lanes.shape[1])
    return jnp.sum(jnp.where(iota(shape, 1) == iota(shape, 0) + start, lanes, 0.0), axis=1, keepdims=True)


def to_lanes(column, start=0, width=128):
    shape = (column.shape[0], width)
    return jnp.sum(jnp.where(iota(shape, 1) == iota(shape, 0) + start, column, 0.0), axis=0, keepdims=True)


def halves(v):
    total = v[:, :128]
    for n in range(128, v.shape[1], 128):
        total = total + v[:, n : n + 128]
    return total


def frame_masks(bounds, frames):
    last = bounds.shape[1] - 1

    def living(f):
        return (f >= 0) & (f < bounds[0, last])

    def paired(f):
        both = living(f) & living(f + 1)
        for k in range(1, last):
            both = both & (f + 1 != bounds[0, k])
        return both

    return tuple(m.astype(F32) for m in (living(frames), paired(frames - 1), paired(frames)))


def row_valid(row, rows):
    mel = lax.axis_index("mel") * rows + row
    return ((mel >= 0) & (mel < lax.axis_size("mel") * rows)).astype(F32)


def start_all(*pairs, sems):
    copies = [pltpu.make_async_copy(src, dst, sems.at[n]) for n, (src, dst) in enumerate(pairs)]
    for copy in copies:
        copy.start()
    return copies


def wait_all(copies):
    for copy in copies:
        copy.wait()


def shifted_frames(value, behind, ahead):
    wide = value.shape[1]
    return pltpu.roll(value, 1, 1) * behind, pltpu.roll(value, wide - 1, 1) * ahead


def three_parts(v):
    high = lax.reduce_precision(v, 8, 7)
    mid = lax.reduce_precision(v - high, 8, 7)
    return high, mid, v - high - mid


def share_of(devices, chan):
    return -(-chan // devices)


def pack(spec_hbm, grad_hbm, bounds_hbm, out, own, spec, masks, bounds, edges, rows_out, sems):
    copies = start_all((bounds_hbm, bounds), (spec_hbm, spec), (grad_hbm, own), sems=sems)
    copies[0].wait()
    wide = masks.shape[1]
    frame_dev = wide - RIM
    devices = out.shape[0]
    rows = MEL_ROWS
    lane = iota((1, wide), 1)
    frames = lax.axis_index("tm") * frame_dev + jnp.where(lane < frame_dev + RIM // 2, lane, lane - wide)
    last = bounds.shape[1] - 1
    pixels = (bounds[0, last] * (lax.axis_size("mel") * rows)).astype(F32)
    found = frame_masks(bounds, frames)
    masks[...] = jnp.concatenate(
        list(found) + [jnp.full((1, wide), 1.0) * pixels, jnp.zeros((4, wide), F32)], axis=0
    )
    usable, behind, ahead = (m[:, :frame_dev] for m in found)
    copies[1].wait()
    x = spec[0].astype(F32) * usable
    lane = iota((1, frame_dev), 1)
    row = iota((rows, 1), 0)
    inner = jnp.where((lane > 0) & (lane < frame_dev - 1), usable, 0.0)
    number = (rows - 2) * jnp.sum(inner, axis=1, keepdims=True)
    inner = inner * ((row > 0) & (row < rows - 1)).astype(F32)
    centre = jnp.sum(jnp.sum(x, axis=0, keepdims=True), axis=1, keepdims=True)
    centre = centre / (rows * jnp.maximum(jnp.sum(usable, axis=1, keepdims=True), 1.0))
    centre = lax.reduce_precision(centre, 8, 7)
    shifted = [pltpu.roll(x, 1, 1) * behind, x, pltpu.roll(x, frame_dev - 1, 1) * ahead]
    taps = [pltpu.roll(v, (1 - i) % rows, 0) if i != 1 else v for i in range(3) for v in shifted]
    features = feature_rows(centre, (taps, inner))
    lane = iota((1, 128), 1)
    features = jnp.where(lane == 90, centre, jnp.where(lane == 91, number, features))
    pick = iota((8, frame_dev), 0)
    column = jnp.where(pick < 4, pick, frame_dev - 8 + pick)
    strip = dot((iota((8, frame_dev), 1) == column).astype(BF16), x.astype(BF16), ((1,), (1,)))
    lane = iota((8, 128), 1)
    repeat = (iota((rows, 128), 1) % rows == iota((rows, 128), 0)).astype(BF16)
    strip = jnp.where(lane // rows == iota((8, 128), 0), dot(strip.astype(BF16), repeat), 0.0)
    strip = jnp.sum(strip, axis=0, keepdims=True)

    def put(n, value):
        rows_out[pl.ds(n, devices, stride=FIRST), :] = jnp.broadcast_to(value, (devices, 128))

    near = jnp.concatenate([x[0:4], x[rows - 4 :]], axis=0)
    near = jnp.concatenate([near[:, :128], near[:, 128:]], axis=0)
    for d in range(devices):
        rows_out[FIRST * d : FIRST * d + 16, :] = near
    put(COLUMNS, strip)
    copies[2].wait()
    _, chan, many, half = own.shape
    share = share_of(devices, chan)
    holders = chan // share
    g = own[0].astype(F32)
    edges[0:chan] = g[:, 0, :]
    edges[chan:] = g[:, many - 1, :]

    def spread_out(v):
        if holders < devices:
            v = jnp.concatenate([v, jnp.zeros((devices - holders, 128), F32)], axis=0)
        return v

    for n in range(share):
        put(EDGES + n, spread_out(edges[n * holders : (n + 1) * holders, :]))
        put(EDGES + share + n, spread_out(edges[chan + n * holders : chan + (n + 1) * holders, :]))
    for n in range(2 * share, COLUMNS - EDGES):
        put(EDGES + n, jnp.zeros((1, 128), F32))
    end = iota((8, half), 0)
    at = iota((8, half), 1)
    ends = ((end == 0) & (at == 0)) | ((end == 1) & (at == half - 1))
    columns = dot(ends.astype(BF16), g.reshape(chan * many, half).astype(BF16), ((1,), (1,)))
    group = 128 // many
    source = iota((128, 128), 0)
    lane = iota((group, 128), 1)
    mine = lane // many == iota((group, 128), 0)
    parts = three_parts(features)
    for n in range(2):
        side = jnp.zeros((holders, 128), F32)
        for m in range(share):
            move = (iota((128, 128), 1) == SIDE + many * m + source % many).astype(BF16)
            first = m * holders * many // 128
            block = [columns[n : n + 1, 128 * q : 128 * (q + 1)] for q in range(first, first + holders * many // 128)]
            block = jnp.concatenate([jnp.where(mine, v, 0.0) for v in block], axis=0)
            side = side + dot(block.astype(BF16), move)
        put(SUMS + n, spread_out(side) + parts[n])
    put(SUMS + 2, parts[2])
    out[...] = rows_out[...].reshape(out.shape).astype(BF16)


def weights(own, bounds_hbm, k2_hbm, k1_hbm, gain_one_hbm, bias_one_hbm, gain_two_hbm, bias_two_hbm,
            wf, wb, w1, ws_hbm, pairs, singles, k1t, params, all_masks, edge_masks, twice, own_rows,
            k2, k1, vectors, bounds, ws, temp, sems):
    loads = start_all(
        (bounds_hbm, bounds),
        (k2_hbm, k2),
        (k1_hbm, k1),
        (gain_one_hbm, vectors.at[0]),
        (bias_one_hbm, vectors.at[1]),
        (gain_two_hbm, vectors.at[2]),
        (bias_two_hbm, vectors.at[3]),
        sems=sems,
    )
    _, many, count, half = own.shape
    temp[...] = own[0].astype(F32).reshape(many * count, half)
    for r in range(count):
        own_rows[r * many : (r + 1) * many] = temp[pl.ds(r, many, stride=count), :].astype(BF16)
    wait_all(loads)
    chan = k2.shape[1]
    span = wf.shape[1]
    taps = [k2[t].astype(F32) for t in range(9)]
    rest = jnp.zeros((chan, span - 9 * chan), F32)
    forward = jnp.concatenate(taps + [rest], axis=1)
    backward = jnp.concatenate([taps[8 - t].T for t in range(9)] + [rest], axis=1)
    for r in range(wb.shape[0] // chan):
        at = slice(r * chan, (r + 1) * chan)
        wb[at] = (pltpu.roll(backward, 3 * chan * r, 1) if r else backward).astype(BF16)
    full = jnp.concatenate([k1[n].astype(F32) for n in range(3)] + [jnp.zeros((7, chan), F32)], axis=0)
    low = [
        jnp.concatenate([full[3 * (2 - a) + 2 - b : 3 * (2 - a) + 3 - b] for a in range(3)], axis=1)
        for b in range(3)
    ]
    rest = jnp.zeros((1, ws.shape[1] - 3 * chan), F32)
    for b in range(3):
        base = jnp.concatenate([low[b], rest], axis=1)
        many = ws.shape[0] // 3
        rolled = [pltpu.roll(base, chan * m, 1) if m else base for m in range(many)]
        ws[many * b : many * (b + 1)] = jnp.concatenate(rolled, axis=0).astype(BF16)
    store_ws = pltpu.make_async_copy(ws, ws_hbm, sems.at[7])
    store_ws.start()
    count, frame_dev = all_masks.shape[0] // 3, all_masks.shape[1]
    frames = iota((count, frame_dev), 0) * frame_dev + iota((count, frame_dev), 1)
    for n, mask in enumerate(frame_masks(bounds, frames)):
        all_masks[n * count : (n + 1) * count] = mask
    q = iota(edge_masks.shape, 0)
    lane = iota(edge_masks.shape, 1)
    k = q % 8
    frames = (q // 8) * frame_dev + jnp.where(k < 4, k, k + frame_dev - 8)
    living, behind, ahead = frame_masks(bounds, frames)
    living = jnp.where((k == 0) | (k == 7), living, 0.0)
    edge_masks[...] = jnp.where(lane == 0, living, jnp.where(lane == 1, behind, jnp.where(lane == 2, ahead, 0.0)))
    params[...] = jnp.concatenate(
        [vectors[n] for n in range(4)] + [jnp.zeros((4, chan), F32)], axis=0
    )
    tap = iota((16, 128), 0)
    lane = iota((16, 128), 1)
    i = (tap * 11) >> 5
    ninth = (lane * 57) >> 9
    to_band = (lane == BAND * (tap - 3 * i) + i) & (tap < 9)
    to_left = (ninth == tap) & (tap < 9)
    to_right = (lane - 9 * ninth == tap) & (lane < 81)
    to_single = (lane == 81 + tap) & (tap < 9)
    source = iota((128, 128), 0) - 81
    lane = iota((128, 128), 1)
    ninth = (lane * 57) >> 9
    inside = (source >= 0) & (source < 9) & (lane < 81)
    twice[...] = jnp.where(inside, (source == ninth).astype(F32) + (source == lane - 9 * ninth).astype(F32), 0.0)
    for r in range(wf.shape[0] // chan):
        at = slice(r * chan, (r + 1) * chan)
        wf[at] = (pltpu.roll(forward, 3 * chan * r, 1) if r else forward).astype(BF16)
    k1t[...] = full
    k = full.astype(BF16)
    lanes = [dot(k, select.astype(BF16), ((0,), (0,))) for select in (to_band, to_left, to_right, to_single)]
    pairs[...] = lanes[1] * lanes[2]
    singles[...] = lanes[3]
    for m in range(w1.shape[0] // chan):
        w1[m * chan : (m + 1) * chan] = (pltpu.roll(lanes[0], m, 1) if m else lanes[0]).astype(BF16)
    store_ws.wait()


def feature_rows(centre, *parts):
    def folded(v):
        return jnp.sum(halves(v), axis=0, keepdims=True)

    rows = [jnp.zeros((1, 128), F32)] * 96
    for taps, weight in parts:
        z = [tap - centre for tap in taps]
        for s in range(9):
            left = z[s] * weight
            rows[81 + s] = rows[81 + s] + folded(left)
            for t in range(s, 9):
                rows[9 * s + t] = rows[9 * t + s] = rows[9 * s + t] + folded(left * z[t])
    return to_lanes(jnp.sum(jnp.concatenate(rows, axis=0), axis=1, keepdims=True))


def summed_blocks(ref, devices):
    block = ref.shape[0] // devices
    period = 8 // math.gcd(block, 8)
    step = period * block
    total = ref[0:step, :]
    for at in range(step, ref.shape[0], step):
        total = total + ref[at : at + step, :]
    result = total[0:block]
    for n in range(1, period):
        result = result + total[n * block : (n + 1) * block]
    return result


def moved_rows(v, step):
    if step == 0:
        return v
    count = v.shape[0]
    if abs(step) >= count:
        return jnp.zeros_like(v)
    zero = jnp.zeros((abs(step), v.shape[1]), v.dtype)
    if step > 0:
        return jnp.concatenate([zero, v[: count - step]], axis=0)
    return jnp.concatenate([v[-step:], zero], axis=0)


def silu_halves(h):
    t = jnp.tanh(h)
    one = 1.0 + t
    return h * one, one * (1.0 + h * (1.0 - t))


def forward_one(recv, spec, pairs, singles, twice, w1, wf, params, masks, all_masks, edge_masks,
                pre_two, payload, act, x3, stats, features_out, pre_one, got, strips, halo, rows_out):
    devices = recv.shape[0]
    n_mel, count = lax.axis_size("mel"), lax.axis_size("tm")
    rows = MEL_ROWS
    mels = n_mel * rows
    wide = masks.shape[1]
    frame_dev = wide - RIM
    chan = params.shape[1]
    me_m, me_t = lax.axis_index("mel"), lax.axis_index("tm")
    usable, behind, ahead = (masks[n : n + 1] for n in range(3))
    total = masks[3:4, 0:1]
    got[...] = recv[...].astype(F32).reshape(devices * FIRST, 128)

    def every(n):
        return got[pl.ds(n, devices, stride=FIRST), :]

    lane = iota((count, 128), 1)
    bands = [got[pl.ds(FIRST * k * count + COLUMNS, count, stride=FIRST), :] for k in range(n_mel)]
    for c in range(8):
        column = jnp.zeros((count, 128), F32)
        for k, band in enumerate(bands):
            part = jnp.where(lane // rows == c, band, 0.0)
            column = column + (pltpu.roll(part, rows * (k - c) % 128, 1) if k != c else part)
        strips[pl.ds(c, count, stride=8), :] = column
    at = pl.multiple_of(FIRST * (jnp.maximum(me_m - 1, 0) * count + me_t), 8)
    above = got[pl.ds(at, 16), :] * (me_m > 0).astype(F32)
    at = pl.multiple_of(FIRST * (jnp.minimum(me_m + 1, n_mel - 1) * count + me_t), 8)
    below = got[pl.ds(at, 16), :] * (me_m < n_mel - 1).astype(F32)
    above = jnp.concatenate([above[4:8], above[12:16]], axis=1)
    below = jnp.concatenate([below[0:4], below[8:12]], axis=1)
    own = spec[0].astype(F32) * usable[:, :frame_dev]
    at = pl.multiple_of(8 * jnp.minimum(me_t + 1, count - 1), 8)
    after = strips[pl.ds(at, 8), :][:, :mels] * (me_t + 1 < count).astype(F32)
    at = pl.multiple_of(8 * jnp.maximum(me_t - 1, 0), 8)
    before = strips[pl.ds(at, 8), :][:, :mels] * (me_t > 0).astype(F32)
    sides = jnp.concatenate([after[0:4], before[4:8], jnp.zeros((8, mels), F32)], axis=0).astype(BF16)
    side = iota((16, RIM), 0)
    place = iota((16, RIM), 1) == jnp.where(side < 4, side, jnp.where(side < 8, side + RIM - 8, -1))
    halo[0:8] = jnp.zeros((8, RIM), F32)
    halo[mels : mels + 8] = jnp.zeros((8, RIM), F32)
    halo[4 : mels + 4] = dot(sides, place.astype(BF16), ((0,), (0,)))
    rim = halo[pl.ds(pl.multiple_of(me_m * rows, 8), BAND), :]
    near = jnp.concatenate([jnp.concatenate([above, own, below], axis=0), rim], axis=1)
    x3[...] = jnp.concatenate(
        [
            pltpu.roll(near, 1, 1) * behind,
            near,
            pltpu.roll(near, wide - 1, 1) * ahead,
            jnp.broadcast_to(usable, (BAND, wide)),
            jnp.zeros((128 - 4 * BAND, wide), F32),
        ],
        axis=0,
    ).astype(BF16)
    pre_one[...] = dot(w1[...], x3[...])
    lane = iota((1, 128), 1)
    parts = jnp.where(lane < 92, every(SUMS) + every(SUMS + 1) + every(SUMS + 2), 0.0)
    centres, numbers = parts[:, 90:91], parts[:, 91:92]
    centre = jnp.sum(centres * numbers, axis=0, keepdims=True)
    centre = centre / jnp.maximum(jnp.sum(numbers, axis=0, keepdims=True), 1.0)
    delta = centres - centre
    features = jnp.sum(parts + delta * numbers * jnp.where(lane < 81, delta, 1.0), axis=0, keepdims=True)
    moved = jnp.sum(delta * parts, axis=0, keepdims=True)
    def edge_row(k, n):
        first = FIRST * k * count + n
        return jnp.concatenate(
            [got[pl.ds(first, count, stride=FIRST), :], got[pl.ds(first + 8, count, stride=FIRST), :]], axis=1
        )

    edge_rows = [[edge_row(k, n) for n in (0, 1, 6, 7)] for k in range(n_mel)]
    zero = jnp.zeros((count, frame_dev), F32)
    rows_of = [[], [], []]
    for k, (top, second, fore, bottom) in enumerate(edge_rows):
        for n, v in enumerate((edge_rows[k - 1][3] if k else zero, top, second)):
            rows_of[n].append(v)
        for n, v in enumerate((fore, bottom, edge_rows[k + 1][0] if k + 1 < n_mel else zero)):
            rows_of[n].append(v)
    f_usable, f_behind, f_ahead = (all_masks[n * count : (n + 1) * count, :] for n in range(3))
    lane = iota((count, frame_dev), 1)

    def frame_before(v):
        v = pltpu.roll(v, 1, 1)
        return jnp.where(lane == 0, pltpu.roll(v, 1, 0), v) * f_behind

    def frame_after(v):
        v = pltpu.roll(v, frame_dev - 1, 1)
        return jnp.where(lane == frame_dev - 1, pltpu.roll(v, count - 1, 0), v) * f_ahead

    taps = []
    for group in rows_of:
        for move in (frame_before, lambda v: v, frame_after):
            taps.append(jnp.concatenate([move(v) for v in group], axis=1))
    f_usable = jnp.concatenate([f_usable] * (2 * n_mel), axis=1)
    borders = (taps, f_usable)
    edge = strips[...]
    q_usable, q_behind, q_ahead = (edge_masks[:, n : n + 1] for n in range(3))
    lane = iota((count * 8, 128), 1)
    inside = (lane < mels) & (lane % rows != 0) & (lane % rows != rows - 1)
    shifted = [
        pltpu.roll(edge, 1, 0) * q_behind,
        edge,
        pltpu.roll(edge, count * 8 - 1, 0) * q_ahead,
    ]
    taps = [pltpu.roll(v, (1 - i) % 128, 1) if i != 1 else v for i in range(3) for v in shifted]
    features = features + feature_rows(centre, borders, (taps, jnp.where(inside, q_usable, 0.0)))
    features = jnp.where(iota((1, 128), 1) < 90, features, 0.0)
    near_mean = jnp.sum(singles[...] * features, axis=1, keepdims=True) / total
    around = jnp.sum(singles[...], axis=1, keepdims=True)
    square = jnp.sum(pairs[...] * features, axis=1, keepdims=True)
    square = (square + 2.0 * around * jnp.sum(singles[...] * moved, axis=1, keepdims=True)) / total
    inv = lax.rsqrt(square - near_mean * near_mean + 1e-05)
    mean = near_mean + centre * around
    lane = iota((chan, 128), 1)
    stats[0:chan] = jnp.where(lane == 0, mean, jnp.where(lane == 1, inv, 0.0))
    stats[chan : chan + 8] = jnp.broadcast_to(to_lanes(near_mean), (8, 128))
    stats[chan + 8 : chan + 16] = jnp.broadcast_to(to_lanes(inv), (8, 128))
    scale = 0.5 * to_column(params[0:1], chan) * inv
    shift = 0.5 * to_column(params[1:2], chan) - mean * scale
    stats[chan + 16 :] = jnp.where(lane == 0, scale, jnp.where(lane == 1, shift, 0.0))
    scale = jnp.broadcast_to(scale, (chan, wide))
    shift = jnp.broadcast_to(shift, (chan, wide))
    ext = w1.shape[0] // chan
    block, taps = wf.shape
    first = jnp.zeros((chan, 128), F32)
    second = jnp.zeros((chan, 128), F32)
    own_mask = usable[:, :frame_dev]
    low_masks = [m.astype(BF16) for m in (usable, behind, ahead)]
    for r in range(ext):
        value, _ = silu_halves(pre_one[r * chan : (r + 1) * chan, :] * scale + shift)
        if not 0 <= r - 3 < rows:
            value = value * row_valid(r - 3, rows)
        base = r * 3 * chan
        low = value.astype(BF16) * low_masks[0]
        act[base : base + chan, :], act[base + 2 * chan : base + 3 * chan, :] = shifted_frames(low, *low_masks[1:])
        act[base + chan : base + 2 * chan, :] = low
        if r < 3 or r % 2 == 0:
            continue
        g = (r - 3) // 2
        result = dot(wf[...], act[g * 3 * block : g * 3 * block + taps, :frame_dev])
        pre_two[g * block : (g + 1) * block, :frame_dev] = result
        if g % 2:
            beside = [act[n * 3 * block : n * 3 * block + taps, frame_dev:] for n in (g - 1, g)]
            beside = dot(wf[...], jnp.concatenate(beside, axis=1))
            for n in range(2):
                pre_two[(g - 1 + n) * block : (g + n) * block, frame_dev:] = beside[:, n * RIM : (n + 1) * RIM]
        for q in range(2):
            if 2 <= 2 * g + q < rows + 2:
                p = result[q * chan : (q + 1) * chan]
                masked = p * own_mask
                first = first + halves(masked)
                second = second + halves(masked * p)
    moved = dot(jnp.broadcast_to(moved, (8, 128)), twice[...], precision=EXACT)[0:1]
    features_out[...] = jnp.concatenate(
        [features + moved, jnp.broadcast_to(centre, (1, 128)), jnp.zeros((6, 128), F32)], axis=0
    )
    share = share_of(devices, chan)

    def put(n, value):
        rows_out[pl.ds(n, devices, stride=SECOND), :] = jnp.broadcast_to(value, (devices, 128))

    for n in range(share):
        put(3 + n, moved_rows(every(EDGES + share + n), count))
        put(3 + share + n, moved_rows(every(EDGES + n), -count))
    for n in [0, 1, 2] + list(range(3 + 2 * share, SECOND - 1)):
        put(n, jnp.zeros((1, 128), F32))
    lane = iota((devices, 128), 1)
    tm = iota((devices, 128), 0) % count
    lefts = jnp.where(lane >= SIDE, every(SUMS), 0.0)
    rights = jnp.where(lane >= SIDE, every(SUMS + 1), 0.0)
    beside = jnp.zeros((devices, 128), F32)
    for n, step in enumerate((0, count, -count)):
        one = jnp.where(tm > 0, moved_rows(rights, step + 1), 0.0)
        two = jnp.where(tm < count - 1, moved_rows(lefts, step - 1), 0.0)
        beside = beside + pltpu.roll(one, (32 * n - SIDE) % 128, 1) + pltpu.roll(two, (32 * n + 16 - SIDE) % 128, 1)
    put(SECOND - 1, beside)
    first = jnp.sum(first, axis=1, keepdims=True)
    second = jnp.sum(second, axis=1, keepdims=True)
    parts = list(three_parts(to_lanes(first) + to_lanes(second, chan)))
    parts = jnp.concatenate(parts + [jnp.zeros((SECOND - 3, 128), F32)], axis=0)
    for d in range(devices):
        payload[d] = (rows_out[SECOND * d : SECOND * (d + 1), :] + parts).astype(BF16)


def sum_rows(devices, taps):
    return -(-taps // devices) + 2


def backward_scaled(recv, pre_two, act, own_rows, params, masks,
                    grad, payload, pairs, stats, sides, up, right, got, beyond):
    devices = recv.shape[0]
    got[...] = recv[...].astype(F32).reshape(devices * SECOND, 128)
    chan = params.shape[1]
    half = own_rows.shape[1]
    lane = iota((half, 2 * half), 1)
    spread = jnp.where(lane >> 1 == iota((half, 2 * half), 0), 0.25, 0.0).astype(BF16)
    rows = MEL_ROWS
    wide = pre_two.shape[1]
    frame_dev = wide - RIM
    usable = masks[0:1]
    share = share_of(devices, chan)
    holders = chan // share

    def every(n):
        return got[pl.ds(n, devices, stride=SECOND), :]

    beside = every(SECOND - 1)[:holders]
    lane = iota((holders, RIM), 1)
    many = rows // 2
    up[0 : many * chan] = dot(own_rows[...], spread)
    for n in range(share):
        first = n * holders
        beyond[first : first + holders, :] = every(3 + n)[:holders]
        beyond[chan + first : chan + first + holders, :] = every(3 + share + n)[:holders]
        for r in range(many + 2):
            at = many * n + (r if r < many else 32 + many - 1 if r == many else 64)
            left, right_of = beside[:, at : at + 1], beside[:, at + 16 : at + 17]
            side = jnp.where(lane >= RIM - 2, 0.25 * left, jnp.where(lane < 2, 0.25 * right_of, 0.0))
            sides[r * chan + first : r * chan + first + holders, :] = side
    up[many * chan :] = dot(beyond[...].astype(BF16), spread)
    total = masks[3:4, 0:1]
    sums = jnp.sum(every(0) + every(1) + every(2), axis=0, keepdims=True)
    mean = to_column(sums, chan) / total
    inv = lax.rsqrt(to_column(sums, chan, chan) / total - mean * mean + 1e-05)
    lane = iota((chan, 128), 1)
    scale = 0.5 * to_column(params[2:3], chan) * inv
    shift = 0.5 * to_column(params[3:4], chan) - mean * scale
    columns = jnp.zeros((chan, 128), F32)
    for n, column in enumerate((mean, inv, scale, shift)):
        columns = jnp.where(lane == n, column, columns)
    stats[0:chan] = columns
    stats[chan : chan + 8] = jnp.broadcast_to(to_lanes(inv), (8, 128))
    shift = jnp.broadcast_to(shift, (chan, wide))
    scale = jnp.broadcast_to(scale, (chan, wide))
    mean = jnp.broadcast_to(mean, (chan, frame_dev))
    inv = jnp.broadcast_to(inv, (chan, frame_dev))
    first = jnp.zeros((chan, 128), F32)
    second = jnp.zeros((chan, 128), F32)
    own_mask = usable[:, :frame_dev]
    right[3 * chan :] = jnp.ones((16, rows * frame_dev), BF16)
    table = jnp.zeros((9 * chan, 3 * chan + 16), F32)
    for q in list(range(2, rows + 2)) + [0, 1, rows + 2, rows + 3]:
        r = q // 2
        at = slice(q * chan, (q + 1) * chan)
        m = q - 2
        mask = 0.5 * usable if 0 <= m < rows else usable * (0.5 * row_valid(m, rows))
        if q % 2 == 0:
            spot = (r - 1 if 1 <= r <= many else many + (r > 0)) * chan
            upstream = jnp.concatenate([up[spot : spot + chan, :], sides[spot : spot + chan, :]], axis=1)
        pre = pre_two[at, :]
        value, slope = silu_halves(pre * scale + shift)
        g = upstream * slope * mask
        grad[at, :] = g
        if not 0 <= m < rows:
            continue
        g = g[:, :frame_dev]
        normed = (pre[:, :frame_dev] - mean) * inv
        first = first + halves(g * normed)
        second = second + halves(g)
        value = value[:, :frame_dev] * own_mask
        both = value if m % 2 == 0 else both + value
        if m % 2:
            pairs[(r - 1) * chan : r * chan, :] = both
        lanes = slice(m * frame_dev, (m + 1) * frame_dev)
        right[0:chan, lanes] = g.astype(BF16)
        right[chan : 2 * chan, lanes] = normed.astype(BF16)
        right[2 * chan : 3 * chan, lanes] = (g - right[0:chan, lanes].astype(F32)).astype(BF16)
        if m in (3, 9, rows - 1):
            start = {3: 0, 9: 4}.get(m, 10)
            left = [act[(n + 2) * 3 * chan : (n + 5) * 3 * chan, :frame_dev] for n in range(start, m + 1)]
            lanes = slice(start * frame_dev, (m + 1) * frame_dev)
            table = table + dot(jnp.concatenate(left, axis=1), right[:, lanes], ((1,), (1,)))
    first = jnp.sum(first, axis=1, keepdims=True)
    second = jnp.sum(second, axis=1, keepdims=True)
    totals = to_lanes(first) + to_lanes(second, chan)
    block = payload.shape[0] // devices
    payload[pl.ds(0, devices, stride=block), :] = jnp.broadcast_to(totals, (devices, 128))
    rest = jnp.concatenate([table[:, 2 * chan :], jnp.zeros((9 * chan, chan - 16), F32)], axis=1)
    both = table[:, : 2 * chan] + jnp.where(iota(rest.shape, 1) < chan, rest, 0.0)
    single = rest[:, chan : chan + 1]
    lane = iota((devices, 128), 1)
    constants = jnp.zeros((devices, 128), F32)
    for k in range(block - 2):
        cut, ones = both[k * devices : (k + 1) * devices], single[k * devices : (k + 1) * devices]
        short = devices - cut.shape[0]
        if short:
            cut = jnp.concatenate([cut, jnp.zeros((short, 128), F32)], axis=0)
            ones = jnp.concatenate([ones, jnp.zeros((short, 1), F32)], axis=0)
        payload[pl.ds(1 + k, devices, stride=block), :] = cut
        constants = jnp.where(lane == k, ones, constants)
    payload[pl.ds(block - 1, devices, stride=block), :] = constants


def pool(totals, pairs, out, gain_out, bias_out, temp):
    gain_out[...] = totals[0:1, : gain_out.shape[1]]
    bias_out[...] = totals[0:1, gain_out.shape[1] :]
    chan, rows, half = out.shape[1:]
    to_mean = jnp.where(iota((2 * half, half), 0) >> 1 == iota((2 * half, half), 1), 0.25, 0.0)
    pooled = dot(pairs[...], to_mean, precision=EXACT)
    for r in range(rows):
        temp[pl.ds(r, chan, stride=rows), :] = pooled[r * chan : (r + 1) * chan]
    out[0] = temp[...].reshape(chan, rows, half).astype(BF16)


def backward(recv, pre_two, grad, stats_two, w1, x3, stats, params, masks, wb,
             out, own_low, payload, totals, g3, pre_one, g1):
    chan = params.shape[1]
    rows = MEL_ROWS
    wide = pre_two.shape[1]
    frame_dev = wide - RIM
    usable = masks[0:1]
    behind, ahead = (masks[n : n + 1].astype(BF16) for n in (1, 2))
    total = masks[3:4, 0:1]
    devices = payload.shape[0] // 14
    pre_one[...] = dot(w1[3 * chan : (rows + 3) * chan], x3[:, :frame_dev])

    received = summed_blocks(recv, devices)
    sums = received[0:1]
    gain_sum, bias_sum = sums[:, :chan], sums[:, chan:]
    totals[...] = jnp.broadcast_to(sums, (8, 128))
    mean, inv = stats_two[0:chan, 0:1], stats_two[0:chan, 1:2]
    factor = to_column(params[2:3], chan) * inv
    gain_part = factor * (to_column(sums, chan) / total * inv)
    bias_part = factor * (to_column(sums, chan, chan) / total) - mean * gain_part
    gain_part = jnp.broadcast_to(gain_part, (chan, wide))
    bias_part = jnp.broadcast_to(bias_part, (chan, wide))
    factor = jnp.broadcast_to(factor, (chan, wide))
    scale = jnp.broadcast_to(stats[chan + 16 :, 0:1], (chan, frame_dev))
    shift = jnp.broadcast_to(stats[chan + 16 :, 1:2], (chan, frame_dev))
    factor_one = jnp.broadcast_to(to_column(params[0:1], chan) * stats[0:chan, 1:2], (chan, frame_dev))
    own_mask = 0.5 * usable[:, :frame_dev]
    count = pre_two.shape[0] // chan
    table = jnp.zeros((chan, 128), F32)

    def tap_sums(m):
        part = g1[m * chan : (m + 4) * chan, :]
        high = lax.reduce_precision(part, 8, 7)
        low = (part - high).astype(BF16)
        taps_in = x3[:, :frame_dev]
        products = dot(high.astype(BF16), taps_in, ((1,), (1,))) + dot(low, taps_in, ((1,), (1,)))
        moved = [pltpu.roll(products[k * chan : (k + 1) * chan], 128 - (m + k + 3), 1) for k in range(4)]
        return (moved[0] + moved[1]) + (moved[2] + moved[3])

    for q in range(count):
        at = slice(q * chan, (q + 1) * chan)
        mask = usable if 0 <= q - 2 < rows else usable * row_valid(q - 2, rows)
        low = (factor * grad[at, :] - (bias_part + pre_two[at, :] * gain_part) * mask).astype(BF16)
        out[at, :] = low
        if not 1 <= q < count - 1:
            continue
        base = (q - 1) * 3 * chan
        for n, v in enumerate((low,) + shifted_frames(low, behind, ahead)):
            spot = base + (1, 0, 2)[n] * chan
            g3[spot : spot + chan, :] = v[:, :frame_dev]
        start = q - 4
        if start < 0 or start % 2:
            continue
        result = dot(wb[...], g3[start * 3 * chan : (start + 4) * 3 * chan, :])
        for n in range(2):
            m = start + n
            at = slice(m * chan, (m + 1) * chan)
            _, slope = silu_halves(pre_one[at, :] * scale + shift)
            value = result[n * chan : (n + 1) * chan] * slope * own_mask
            own_low[at, :] = (value * factor_one).astype(BF16)
            g1[at, :] = value
        if start % 4 == 2 and start > 2:
            table = table + tap_sums(start - 6)
    table = table + tap_sums(rows - 4)
    table = table.T
    places = [BAND * j + i for i in range(3) for j in range(3)] + [3 * BAND]
    rows10 = jnp.concatenate([table[n : n + 1] for n in places], axis=0)
    share = received.shape[0] - 2
    mine = received[1 : share + 1]
    single = to_column(received[share + 1 :], share)
    factor_l = params[2:3] * stats_two[chan : chan + 1, :chan]
    mine = mine[:, :chan] - (bias_sum * single + gain_sum * mine[:, chan:]) / total
    mine = factor_l * mine
    lower = -(-share // 2)
    mine = jnp.concatenate([mine] + [jnp.zeros((2 * lower - share, chan), F32)] * (share % 2), axis=0)
    mine = jnp.concatenate([mine[:lower], mine[lower:]], axis=1)
    if lower < 9:
        mine = jnp.concatenate([mine, jnp.zeros((9 - lower, 128), F32)], axis=0)
    sums = jnp.concatenate([rows10[0:5], rows10[5:10]], axis=1)
    block = jnp.concatenate([sums, mine], axis=0)
    block = jnp.concatenate([block] * 4, axis=0)
    for d in range(0, devices, 4):
        payload[14 * d : 14 * (d + 4), :] = block


def transposed(grad, own_low, w1, wb, x3, stats, features, k1t, params, masks, ws_hbm,
               first, ws, normed_taps, low, g3, rim, sem):
    load = pltpu.make_async_copy(ws_hbm, ws, sem)
    load.start()
    rows = MEL_ROWS
    chan = own_low.shape[0] // rows
    wide = grad.shape[1]
    frame_dev = wide - RIM
    count = grad.shape[0] // chan
    usable = masks[0:1]
    behind, ahead = (masks[n : n + 1].astype(BF16) for n in (1, 2))
    scale = jnp.broadcast_to(stats[chan + 16 :, 0:1], (chan, wide))
    shift = jnp.broadcast_to(stats[chan + 16 :, 1:2], (chan, wide))
    factor = jnp.broadcast_to(to_column(params[0:1], chan) * stats[0:chan, 1:2], (chan, wide))
    edge = (0, 1, 2, 3, count - 4, count - 3, count - 2, count - 1)
    for q in range(count):
        value = grad[q * chan : (q + 1) * chan, :]
        for n, v in enumerate((value,) + shifted_frames(value, behind, ahead)):
            spot = (3 * q + (1, 0, 2)[n]) * chan
            rim[spot : spot + chan, :] = v[:, frame_dev:]
            if q in edge:
                spot = (3 * edge.index(q) + (1, 0, 2)[n]) * chan
                g3[spot : spot + chan, :] = v[:, :frame_dev]
    low[chan : (rows + 1) * chan, :frame_dev] = own_low[...]

    def put(m, lanes, result, pre_one):
        at = slice((m + 1) * chan, (m + 2) * chan)
        _, slope = silu_halves(pre_one * scale[:, lanes] + shift[:, lanes])
        mask = usable[:, lanes] * (0.5 * row_valid(m, rows))
        low[at, lanes] = (result * slope * mask * factor[:, lanes]).astype(BF16)

    pre_one = dot(w1[2 * chan : (rows + 4) * chan, :], x3[:, frame_dev:])
    beside = slice(frame_dev, wide)
    for start in range(0, rows + 2, 2):
        result = dot(wb[...], rim[start * 3 * chan : (start + 4) * 3 * chan, :])
        for n in range(2):
            at = slice((start + n) * chan, (start + n + 1) * chan)
            put(start + n - 1, beside, result[n * chan : (n + 1) * chan], pre_one[at])
    own = slice(0, frame_dev)
    result = dot(wb[...], g3[: 4 * 3 * chan, :])
    put(-1, own, result[:chan], dot(w1[2 * chan : 3 * chan, :], x3[:, :frame_dev]))
    result = dot(wb[...], g3[4 * 3 * chan :, :])
    put(rows, own, result[chan:], dot(w1[(rows + 3) * chan : (rows + 4) * chan, :], x3[:, :frame_dev]))
    row = features[0:1, :]
    lane = iota((1, 128), 1)
    gram = jnp.concatenate(
        [jnp.where(lane < 9, pltpu.roll(row, 128 - 9 * t, 1) if t else row, 0.0) for t in range(9)]
        + [jnp.zeros((7, 128), F32)],
        axis=0,
    )
    single = to_column(row, 16, 81)[0:9]
    k_rows = jnp.concatenate([k1t[...], jnp.zeros((112, chan), F32)], axis=0)
    mean_l, inv_l = stats[chan : chan + 1, :chan], stats[chan + 8 : chan + 9, :chan]
    normed = inv_l * (dot(gram, k_rows, precision=EXACT)[0:9] - single * mean_l)
    normed_taps[0:16] = jnp.concatenate([normed, jnp.zeros((7, chan), F32)], axis=0)
    normed_taps[16:32] = jnp.broadcast_to(to_column(row, 16, 81), (16, chan))
    load.wait()
    first[...] = dot(ws[...], low[...])


def finish(recv, features, stats, k1t, first, ws, w1, x3, normed_taps, params, masks,
           spec_hbm, kernel_one_hbm, kernel_two_hbm, gain_hbm, bias_hbm,
           spec_grad, kernel_one, kernel_two, gain_out, bias_out, sems):
    chan = params.shape[1]
    rows = MEL_ROWS
    wide = x3.shape[1]
    frame_dev = wide - RIM
    usable, behind, ahead = (masks[n : n + 1] for n in range(3))
    total = masks[3:4, 0:1]
    gain = params[0:1]
    count = recv.shape[0] // 14
    share = -(-9 * chan // count)
    lower = -(-share // 2)
    left = [recv[pl.ds(5 + p, count, stride=14), :] for p in range(lower)]
    whole = jnp.concatenate([v[:, :chan] for v in left] + [v[:, chan:] for v in left], axis=0)
    for t in range(9):
        kernel_two[t] = whole[t * chan : (t + 1) * chan].T
    stores = [pltpu.make_async_copy(kernel_two, kernel_two_hbm, sems.at[4])]
    stores[0].start()
    sums = summed_blocks(recv, count)[0:5]
    ten = jnp.concatenate([sums[:, :chan], sums[:, chan:]], axis=0)
    bias_sum = ten[9:10]
    mean_l, inv_l = stats[chan : chan + 1, :chan], stats[chan + 8 : chan + 9, :chan]
    ten = ten - features[1:2, 0:1] * bias_sum
    k = k1t[0:9]
    gain_sum = inv_l * (jnp.sum(k * ten[0:9], axis=0, keepdims=True) - mean_l * bias_sum)
    gain_out[...] = gain_sum
    bias_out[...] = bias_sum
    factor_l = gain * inv_l
    scale = factor_l * gain_sum / total * inv_l
    scale = jnp.concatenate(
        [scale * row_valid(-1, rows)] + [scale] * rows + [scale * row_valid(rows, rows)], axis=1
    )
    many = 3 * rows

    def in_parts(v, right):
        high = lax.reduce_precision(v, 8, 7)
        v = dot(jnp.concatenate([high, v - high], axis=0).astype(BF16), right)
        return v[:many] + v[many:]

    taken = in_parts(in_parts(ws[...].astype(F32) * scale, w1[2 * chan : (rows + 4) * chan, :]), x3[...])
    taps = first[...] - taken
    moved = [taps[rows * b : rows * (b + 1)] for b in range(3)]
    mean_full = mean_l + features[1:2, 0:1] * jnp.sum(k, axis=0, keepdims=True)
    constant = jnp.sum(k * (factor_l * (bias_sum - gain_sum * inv_l * mean_full) / total), axis=1, keepdims=True)
    for a in range(3):
        row = iota((rows, 1), 0) + (a - 1) + lax.axis_index("mel") * rows
        valid = ((row >= 0) & (row < lax.axis_size("mel") * rows)).astype(F32) * usable
        for b in range(3):
            t = 3 * (2 - a) + 2 - b
            moved[b] = moved[b] - constant[t : t + 1] * valid
    result = pltpu.roll(moved[0], 1, 1) * behind + moved[1] + pltpu.roll(moved[2], wide - 1, 1) * ahead
    spec_grad[0] = (result * usable)[:, :frame_dev]
    grad_taps = factor_l * (ten[0:9] - (bias_sum * normed_taps[16:25] + gain_sum * normed_taps[0:9]) / total)
    for i in range(3):
        kernel_one[i] = grad_taps[3 * i : 3 * i + 3]
    outs = ((spec_grad, spec_hbm), (kernel_one, kernel_one_hbm), (gain_out, gain_hbm), (bias_out, bias_hbm))
    wait_all(stores + start_all(*outs, sems=sems))


def run(kernel, outs, scratch, *args, hbm=0, apart=(), flops=10**8, size=4 * 10**6):
    vmem = pl.BlockSpec(memory_space=pltpu.VMEM)
    devices = lax.axis_size("mel") * lax.axis_size("tm")
    specs = []
    args = list(args)
    for n, a in enumerate(args):
        if hbm and n >= len(args) - hbm:
            specs.append(pl.BlockSpec(memory_space=pltpu.HBM))
            args[n] = pltpu.with_memory_space_constraint(a, pltpu.HBM)
        else:
            specs.append(vmem)
            args[n] = pltpu.with_memory_space_constraint(a, pltpu.VMEM)
    return pl.pallas_call(
        kernel,
        out_shape=outs,
        in_specs=specs,
        out_specs=[pl.BlockSpec(memory_space=pltpu.HBM) if n in apart else vmem for n in range(len(outs))],
        scratch_shapes=scratch,
        compiler_params=pltpu.CompilerParams(vmem_limit_bytes=(29 + devices // 32) * 2**20),
        cost_estimate=pl.CostEstimate(flops=flops, bytes_accessed=size, transcendentals=0),
    )(*args)


def shape(dims, dtype=F32):
    return jax.ShapeDtypeStruct(dims, dtype)


def kept(dims, dtype=F32):
    return pltpu.VMEM(dims, dtype)


def far(dims, dtype=F32):
    return pltpu.HBM(dims, dtype)


def exchange(blocks, axes=AXES):
    return lax.all_to_all(blocks, axes, 0, 0, tiled=True)


def exchange_rows(rows, axes=AXES):
    return exchange(rows[:, None, :], axes)[:, 0, :]


def shards(spectrum, clip_bounds, kernel_one, gain_one, bias_one, kernel_two, gain_two, bias_two, pooled_grad):
    _, rows, frame_dev = spectrum.shape
    chan = kernel_two.shape[0]
    n_mel, n_tm = lax.axis_size("mel"), lax.axis_size("tm")
    devices = n_mel * n_tm
    half = frame_dev // 2
    wide = frame_dev + RIM
    mels = n_mel * rows

    packed, own, spec, masks = run(
        pack,
        [
            kept((devices, FIRST, 128), BF16),
            kept(pooled_grad.shape, BF16),
            kept(spectrum.shape, BF16),
            kept((8, wide)),
        ],
        [
            pltpu.SMEM(clip_bounds.shape, jnp.int32),
            pltpu.VMEM((2 * chan, half), F32),
            pltpu.VMEM((devices * FIRST, 128), F32),
            pltpu.SemaphoreType.DMA((3,)),
        ],
        spectrum,
        pooled_grad,
        clip_bounds,
        hbm=3,
    )
    recv = exchange(packed)
    ext = rows + 6
    span = 4 * 3 * chan
    wf, wb, w1, ws, pairs, singles, k1t, params, all_masks, edge_masks, twice, own_rows = run(
        weights,
        [
            kept((2 * chan, span), BF16),
            kept((2 * chan, span), BF16),
            kept((ext * chan, 128), BF16),
            far((rows * 3, (rows + 2) * chan), BF16),
            kept((chan, 128)),
            kept((chan, 128)),
            kept((16, chan)),
            kept((8, chan)),
            kept((3 * n_tm, frame_dev)),
            kept((n_tm * 8, 128)),
            kept((128, 128)),
            kept((chan * rows // 2, half), BF16),
        ],
        [
            pltpu.VMEM((9, chan, chan), BF16),
            pltpu.VMEM((3, 3, chan), BF16),
            pltpu.VMEM((4, 1, chan), F32),
            pltpu.SMEM(clip_bounds.shape, jnp.int32),
            pltpu.VMEM((rows * 3, (rows + 2) * chan), BF16),
            pltpu.VMEM((chan * rows // 2, half), F32),
            pltpu.SemaphoreType.DMA((8,)),
        ],
        own,
        clip_bounds,
        jnp.transpose(kernel_two, (2, 3, 0, 1)).reshape(9, chan, chan),
        jnp.transpose(kernel_one, (1, 2, 0)),
        gain_one[None],
        bias_one[None],
        gain_two[None],
        bias_two[None],
        hbm=7,
        apart=(3,),
    )
    pre_two, payload, act, x3, stats_one, features = run(
        forward_one,
        [
            kept(((rows + 4) * chan, wide)),
            kept((devices, SECOND, 128), BF16),
            kept((ext * 3 * chan, wide), BF16),
            kept((128, wide), BF16),
            kept((2 * chan + 16, 128)),
            kept((8, 128)),
        ],
        [
            pltpu.VMEM((ext * chan, wide), F32),
            pltpu.VMEM((devices * FIRST, 128), F32),
            pltpu.VMEM((n_tm * 8, 128), F32),
            pltpu.VMEM((mels + 8, RIM), F32),
            pltpu.VMEM((devices * SECOND, 128), F32),
        ],
        recv,
        spec,
        pairs,
        singles,
        twice,
        w1,
        wf,
        params,
        masks,
        all_masks,
        edge_masks,
    )
    recv = exchange(payload)
    grad, payload, row_pairs, stats_two = run(
        backward_scaled,
        [
            kept(((rows + 4) * chan, wide)),
            kept((devices * sum_rows(devices, 9 * chan), 128)),
            kept((rows // 2 * chan, frame_dev)),
            kept((chan + 8, 128)),
        ],
        [
            pltpu.VMEM(((rows // 2 + 2) * chan, RIM), F32),
            pltpu.VMEM(((rows // 2 + 2) * chan, frame_dev), F32),
            pltpu.VMEM((3 * chan + 16, rows * frame_dev), BF16),
            pltpu.VMEM((devices * SECOND, 128), F32),
            pltpu.VMEM((2 * chan, half), F32),
        ],
        recv,
        pre_two,
        act,
        own_rows,
        params,
        masks,
    )
    recv = exchange_rows(payload)
    grad, own_low, payload, totals = run(
        backward,
        [
            kept(((rows + 4) * chan, wide), BF16),
            kept((rows * chan, frame_dev), BF16),
            kept((devices * 14, 128)),
            kept((8, 128)),
        ],
        [
            pltpu.VMEM(((rows + 2) * 3 * chan, frame_dev), BF16),
            pltpu.VMEM((rows * chan, frame_dev), F32),
            pltpu.VMEM((rows * chan, frame_dev), F32),
        ],
        recv,
        pre_two,
        grad,
        stats_two,
        w1,
        x3,
        stats_one,
        params,
        masks,
        wb,
    )
    recv = exchange_rows(payload)
    pooled, gain_two_grad, bias_two_grad = run(
        pool,
        [shape((1, chan, rows // 2, half), BF16), shape((1, chan)), shape((1, chan))],
        [
            pltpu.VMEM((rows // 2 * chan, 128), F32),
        ],
        totals,
        row_pairs,
    )
    first, ws, normed_taps = run(
        transposed,
        [
            kept((rows * 3, wide)),
            kept((rows * 3, (rows + 2) * chan), BF16),
            kept((32, chan)),
        ],
        [
            pltpu.VMEM(((rows + 2) * chan, wide), BF16),
            pltpu.VMEM((8 * 3 * chan, frame_dev), BF16),
            pltpu.VMEM(((rows + 4) * 3 * chan, RIM), BF16),
            pltpu.SemaphoreType.DMA,
        ],
        grad,
        own_low,
        w1,
        wb,
        x3,
        stats_one,
        features,
        k1t,
        params,
        masks,
        ws,
        hbm=1,
    )
    spec_grad, kernel_one_grad, kernel_two_grad, gain_one_grad, bias_one_grad = run(
        finish,
        [
            shape((1, rows, frame_dev)),
            shape((3, 3, chan)),
            shape((9, chan, chan)),
            shape((1, chan)),
            shape((1, chan)),
        ],
        [
            pltpu.VMEM((1, rows, frame_dev), F32),
            pltpu.VMEM((3, 3, chan), F32),
            pltpu.VMEM((9, chan, chan), F32),
            pltpu.VMEM((1, chan), F32),
            pltpu.VMEM((1, chan), F32),
            pltpu.SemaphoreType.DMA((5,)),
        ],
        recv,
        features,
        stats_one,
        k1t,
        first,
        ws,
        w1,
        x3,
        normed_taps,
        params,
        masks,
        apart=range(5),
    )
    kernel_two_grad = jnp.transpose(kernel_two_grad.reshape(3, 3, chan, chan), (2, 3, 0, 1))
    return (
        pooled,
        spec_grad,
        jnp.transpose(kernel_one_grad, (2, 0, 1)),
        gain_one_grad[0],
        bias_one_grad[0],
        kernel_two_grad,
        gain_two_grad[0],
        bias_two_grad[0],
    )


def solution(mesh):
    return jax.shard_map(
        shards,
        mesh=mesh,
        in_specs=(
            P(None, "mel", "tm"),
            P(),
            P(),
            P(),
            P(),
            P(),
            P(),
            P(),
            P(None, None, "mel", "tm"),
        ),
        out_specs=(P(None, None, "mel", "tm"), P(None, "mel", "tm"), P(), P(), P(), P(), P(), P()),
        check_vma=False,
    )
```

```python
import math

import jax
import jax.numpy as jnp
from jax import lax
from jax.experimental import pallas as pl
from jax.experimental.pallas import tpu as pltpu
from jax.sharding import PartitionSpec as P

F32 = jnp.float32
BF16 = jnp.bfloat16
AXES = ("mel", "tm")
EXACT = lax.Precision.HIGHEST
RIM = 128
BAND = 24
MEL_ROWS = 16
FIRST = 24
SUMS, EDGES, COLUMNS = 16, 19, 23
SIDE = 96
TAPS = 576
SECOND = 8


def iota(shape, dim):
    return lax.broadcasted_iota(jnp.int32, shape, dim)


def dot(a, b, over=((1,), (0,)), precision=None):
    return lax.dot_general(a, b, (over, ((), ())), precision=precision, preferred_element_type=F32)


def to_column(lanes, count, start=0):
    shape = (count, lanes.shape[1])
    return jnp.sum(jnp.where(iota(shape, 1) == iota(shape, 0) + start, lanes, 0.0), axis=1, keepdims=True)


def to_lanes(column, start=0, width=128):
    shape = (column.shape[0], width)
    return jnp.sum(jnp.where(iota(shape, 1) == iota(shape, 0) + start, column, 0.0), axis=0, keepdims=True)


def halves(v):
    total = v[:, :128]
    for n in range(128, v.shape[1], 128):
        total = total + v[:, n : n + 128]
    return total


def frame_masks(bounds, frames):
    last = bounds.shape[1] - 1

    def living(f):
        return (f >= 0) & (f < bounds[0, last])

    def paired(f):
        both = living(f) & living(f + 1)
        for k in range(1, last):
            both = both & (f + 1 != bounds[0, k])
        return both

    return tuple(m.astype(F32) for m in (living(frames), paired(frames - 1), paired(frames)))


def row_valid(row, rows):
    mel = lax.axis_index("mel") * rows + row
    return ((mel >= 0) & (mel < lax.axis_size("mel") * rows)).astype(F32)


def start_all(*pairs, sems):
    copies = [pltpu.make_async_copy(src, dst, sems.at[n]) for n, (src, dst) in enumerate(pairs)]
    for copy in copies:
        copy.start()
    return copies


def wait_all(copies):
    for copy in copies:
        copy.wait()


def shifted_frames(value, behind, ahead):
    wide = value.shape[1]
    return pltpu.roll(value, 1, 1) * behind, pltpu.roll(value, wide - 1, 1) * ahead


def three_parts(v):
    high = lax.reduce_precision(v, 8, 7)
    mid = lax.reduce_precision(v - high, 8, 7)
    return high, mid, v - high - mid


def share_of(devices, chan):
    return -(-chan // devices)


def pack(spec_hbm, grad_hbm, bounds_hbm, out, own, spec, masks, bounds, edges, rows_out, sems):
    copies = start_all((bounds_hbm, bounds), (spec_hbm, spec), (grad_hbm, own), sems=sems)
    copies[0].wait()
    wide = masks.shape[1]
    frame_dev = wide - RIM
    devices = out.shape[0]
    rows = MEL_ROWS
    lane = iota((1, wide), 1)
    frames = lax.axis_index("tm") * frame_dev + jnp.where(lane < frame_dev + RIM // 2, lane, lane - wide)
    last = bounds.shape[1] - 1
    pixels = (bounds[0, last] * (lax.axis_size("mel") * rows)).astype(F32)
    found = frame_masks(bounds, frames)
    masks[...] = jnp.concatenate(
        list(found) + [jnp.full((1, wide), 1.0) * pixels, jnp.zeros((4, wide), F32)], axis=0
    )
    usable, behind, ahead = (m[:, :frame_dev] for m in found)
    copies[1].wait()
    x = spec[0].astype(F32) * usable
    lane = iota((1, frame_dev), 1)
    row = iota((rows, 1), 0)
    inner = jnp.where((lane > 0) & (lane < frame_dev - 1), usable, 0.0)
    number = (rows - 2) * jnp.sum(inner, axis=1, keepdims=True)
    inner = inner * ((row > 0) & (row < rows - 1)).astype(F32)
    centre = jnp.sum(jnp.sum(x, axis=0, keepdims=True), axis=1, keepdims=True)
    centre = centre / (rows * jnp.maximum(jnp.sum(usable, axis=1, keepdims=True), 1.0))
    centre = lax.reduce_precision(centre, 8, 7)
    shifted = [pltpu.roll(x, 1, 1) * behind, x, pltpu.roll(x, frame_dev - 1, 1) * ahead]
    taps = [pltpu.roll(v, (1 - i) % rows, 0) if i != 1 else v for i in range(3) for v in shifted]
    features = feature_rows(centre, (taps, inner))
    lane = iota((1, 128), 1)
    features = jnp.where(lane == 90, centre, jnp.where(lane == 91, number, features))
    pick = iota((8, frame_dev), 0)
    column = jnp.where(pick < 4, pick, frame_dev - 8 + pick)
    strip = dot((iota((8, frame_dev), 1) == column).astype(BF16), x.astype(BF16), ((1,), (1,)))
    lane = iota((8, 128), 1)
    repeat = (iota((rows, 128), 1) % rows == iota((rows, 128), 0)).astype(BF16)
    strip = jnp.where(lane // rows == iota((8, 128), 0), dot(strip.astype(BF16), repeat), 0.0)
    strip = jnp.sum(strip, axis=0, keepdims=True)

    def put(n, value):
        rows_out[pl.ds(n, devices, stride=FIRST), :] = jnp.broadcast_to(value, (devices, 128))

    near = jnp.concatenate([x[0:4], x[rows - 4 :]], axis=0)
    near = jnp.concatenate([near[:, :128], near[:, 128:]], axis=0)
    for d in range(devices):
        rows_out[FIRST * d : FIRST * d + 16, :] = near
    put(COLUMNS, strip)
    copies[2].wait()
    _, chan, many, half = own.shape
    share = share_of(devices, chan)
    holders = chan // share
    g = own[0].astype(F32)
    edges[0:chan] = g[:, 0, :]
    edges[chan:] = g[:, many - 1, :]

    def spread_out(v):
        if holders < devices:
            v = jnp.concatenate([v, jnp.zeros((devices - holders, 128), F32)], axis=0)
        return v

    for n in range(share):
        put(EDGES + n, spread_out(edges[n * holders : (n + 1) * holders, :]))
        put(EDGES + share + n, spread_out(edges[chan + n * holders : chan + (n + 1) * holders, :]))
    for n in range(2 * share, COLUMNS - EDGES):
        put(EDGES + n, jnp.zeros((1, 128), F32))
    end = iota((8, half), 0)
    at = iota((8, half), 1)
    ends = ((end == 0) & (at == 0)) | ((end == 1) & (at == half - 1))
    columns = dot(ends.astype(BF16), g.reshape(chan * many, half).astype(BF16), ((1,), (1,)))
    group = 128 // many
    source = iota((128, 128), 0)
    lane = iota((group, 128), 1)
    mine = lane // many == iota((group, 128), 0)
    parts = three_parts(features)
    for n in range(2):
        side = jnp.zeros((holders, 128), F32)
        for m in range(share):
            move = (iota((128, 128), 1) == SIDE + many * m + source % many).astype(BF16)
            first = m * holders * many // 128
            block = [columns[n : n + 1, 128 * q : 128 * (q + 1)] for q in range(first, first + holders * many // 128)]
            block = jnp.concatenate([jnp.where(mine, v, 0.0) for v in block], axis=0)
            side = side + dot(block.astype(BF16), move)
        put(SUMS + n, spread_out(side) + parts[n])
    put(SUMS + 2, parts[2])
    out[...] = rows_out[...].reshape(out.shape).astype(BF16)


def weights(own, bounds_hbm, k2_hbm, k1_hbm, gain_one_hbm, bias_one_hbm, gain_two_hbm, bias_two_hbm,
            wf, wb, w1, ws_hbm, pairs, singles, k1t, params, all_masks, edge_masks, twice, own_rows,
            k2, k1, vectors, bounds, ws, temp, sems):
    loads = start_all(
        (bounds_hbm, bounds),
        (k2_hbm, k2),
        (k1_hbm, k1),
        (gain_one_hbm, vectors.at[0]),
        (bias_one_hbm, vectors.at[1]),
        (gain_two_hbm, vectors.at[2]),
        (bias_two_hbm, vectors.at[3]),
        sems=sems,
    )
    _, many, count, half = own.shape
    temp[...] = own[0].astype(F32).reshape(many * count, half)
    for r in range(count):
        own_rows[r * many : (r + 1) * many] = temp[pl.ds(r, many, stride=count), :].astype(BF16)
    wait_all(loads)
    chan = k2.shape[1]
    span = wf.shape[1]
    taps = [k2[t].astype(F32) for t in range(9)]
    rest = jnp.zeros((chan, span - 9 * chan), F32)
    forward = jnp.concatenate(taps + [rest], axis=1)
    backward = jnp.concatenate([taps[8 - t].T for t in range(9)] + [rest], axis=1)
    for r in range(wb.shape[0] // chan):
        at = slice(r * chan, (r + 1) * chan)
        wb[at] = (pltpu.roll(backward, 3 * chan * r, 1) if r else backward).astype(BF16)
    full = jnp.concatenate([k1[n].astype(F32) for n in range(3)] + [jnp.zeros((7, chan), F32)], axis=0)
    low = [
        jnp.concatenate([full[3 * (2 - a) + 2 - b : 3 * (2 - a) + 3 - b] for a in range(3)], axis=1)
        for b in range(3)
    ]
    rest = jnp.zeros((1, ws.shape[1] - 3 * chan), F32)
    for b in range(3):
        base = jnp.concatenate([low[b], rest], axis=1)
        many = ws.shape[0] // 3
        rolled = [pltpu.roll(base, chan * m, 1) if m else base for m in range(many)]
        ws[many * b : many * (b + 1)] = jnp.concatenate(rolled, axis=0).astype(BF16)
    store_ws = pltpu.make_async_copy(ws, ws_hbm, sems.at[7])
    store_ws.start()
    count, frame_dev = all_masks.shape[0] // 3, all_masks.shape[1]
    frames = iota((count, frame_dev), 0) * frame_dev + iota((count, frame_dev), 1)
    for n, mask in enumerate(frame_masks(bounds, frames)):
        all_masks[n * count : (n + 1) * count] = mask
    q = iota(edge_masks.shape, 0)
    lane = iota(edge_masks.shape, 1)
    k = q % 8
    frames = (q // 8) * frame_dev + jnp.where(k < 4, k, k + frame_dev - 8)
    living, behind, ahead = frame_masks(bounds, frames)
    living = jnp.where((k == 0) | (k == 7), living, 0.0)
    edge_masks[...] = jnp.where(lane == 0, living, jnp.where(lane == 1, behind, jnp.where(lane == 2, ahead, 0.0)))
    params[...] = jnp.concatenate(
        [vectors[n] for n in range(4)] + [jnp.zeros((4, chan), F32)], axis=0
    )
    tap = iota((16, 128), 0)
    lane = iota((16, 128), 1)
    i = (tap * 11) >> 5
    ninth = (lane * 57) >> 9
    to_band = (lane == BAND * (tap - 3 * i) + i) & (tap < 9)
    to_left = (ninth == tap) & (tap < 9)
    to_right = (lane - 9 * ninth == tap) & (lane < 81)
    to_single = (lane == 81 + tap) & (tap < 9)
    source = iota((128, 128), 0) - 81
    lane = iota((128, 128), 1)
    ninth = (lane * 57) >> 9
    inside = (source >= 0) & (source < 9) & (lane < 81)
    twice[...] = jnp.where(inside, (source == ninth).astype(F32) + (source == lane - 9 * ninth).astype(F32), 0.0)
    for r in range(wf.shape[0] // chan):
        at = slice(r * chan, (r + 1) * chan)
        wf[at] = (pltpu.roll(forward, 3 * chan * r, 1) if r else forward).astype(BF16)
    k1t[...] = full
    k = full.astype(BF16)
    lanes = [dot(k, select.astype(BF16), ((0,), (0,))) for select in (to_band, to_left, to_right, to_single)]
    pairs[...] = lanes[1] * lanes[2]
    singles[...] = lanes[3]
    for m in range(w1.shape[0] // chan):
        w1[m * chan : (m + 1) * chan] = (pltpu.roll(lanes[0], m, 1) if m else lanes[0]).astype(BF16)
    store_ws.wait()


def feature_rows(centre, *parts):
    def folded(v):
        return jnp.sum(halves(v), axis=0, keepdims=True)

    rows = [jnp.zeros((1, 128), F32)] * 96
    for taps, weight in parts:
        z = [tap - centre for tap in taps]
        for s in range(9):
            left = z[s] * weight
            rows[81 + s] = rows[81 + s] + folded(left)
            for t in range(s, 9):
                rows[9 * s + t] = rows[9 * t + s] = rows[9 * s + t] + folded(left * z[t])
    return to_lanes(jnp.sum(jnp.concatenate(rows, axis=0), axis=1, keepdims=True))


def summed_blocks(ref, devices, by=1):
    block = ref.shape[0] // devices
    period = max(8 // math.gcd(block, 8), by)
    step = period * block
    total = ref[0:step, :]
    for at in range(step, ref.shape[0], step):
        total = total + ref[at : at + step, :]
    results = []
    for first in range(by):
        result = total[first * block : (first + 1) * block]
        for n in range(first + by, period, by):
            result = result + total[n * block : (n + 1) * block]
        results.append(result)
    return results if by > 1 else results[0]


def moved_rows(v, step):
    if step == 0:
        return v
    count = v.shape[0]
    if abs(step) >= count:
        return jnp.zeros_like(v)
    zero = jnp.zeros((abs(step), v.shape[1]), v.dtype)
    if step > 0:
        return jnp.concatenate([zero, v[: count - step]], axis=0)
    return jnp.concatenate([v[-step:], zero], axis=0)


def silu_halves(h):
    t = jnp.tanh(h)
    one = 1.0 + t
    return h * one, one * (1.0 + h * (1.0 - t))


def forward_one(recv, spec, pairs, singles, twice, w1, wf, params, masks, all_masks, edge_masks,
                pre_two, payload, act, x3, stats, features_out, pre_one, got, strips, halo, rows_out):
    devices = recv.shape[0]
    n_mel, count = lax.axis_size("mel"), lax.axis_size("tm")
    rows = MEL_ROWS
    mels = n_mel * rows
    wide = masks.shape[1]
    frame_dev = wide - RIM
    chan = params.shape[1]
    me_m, me_t = lax.axis_index("mel"), lax.axis_index("tm")
    usable, behind, ahead = (masks[n : n + 1] for n in range(3))
    total = masks[3:4, 0:1]
    got[...] = recv[...].astype(F32).reshape(devices * FIRST, 128)

    def every(n):
        return got[pl.ds(n, devices, stride=FIRST), :]

    lane = iota((count, 128), 1)
    bands = [got[pl.ds(FIRST * k * count + COLUMNS, count, stride=FIRST), :] for k in range(n_mel)]
    for c in range(8):
        column = jnp.zeros((count, 128), F32)
        for k, band in enumerate(bands):
            part = jnp.where(lane // rows == c, band, 0.0)
            column = column + (pltpu.roll(part, rows * (k - c) % 128, 1) if k != c else part)
        strips[pl.ds(c, count, stride=8), :] = column
    at = pl.multiple_of(FIRST * (jnp.maximum(me_m - 1, 0) * count + me_t), 8)
    above = got[pl.ds(at, 16), :] * (me_m > 0).astype(F32)
    at = pl.multiple_of(FIRST * (jnp.minimum(me_m + 1, n_mel - 1) * count + me_t), 8)
    below = got[pl.ds(at, 16), :] * (me_m < n_mel - 1).astype(F32)
    above = jnp.concatenate([above[4:8], above[12:16]], axis=1)
    below = jnp.concatenate([below[0:4], below[8:12]], axis=1)
    own = spec[0].astype(F32) * usable[:, :frame_dev]
    at = pl.multiple_of(8 * jnp.minimum(me_t + 1, count - 1), 8)
    after = strips[pl.ds(at, 8), :][:, :mels] * (me_t + 1 < count).astype(F32)
    at = pl.multiple_of(8 * jnp.maximum(me_t - 1, 0), 8)
    before = strips[pl.ds(at, 8), :][:, :mels] * (me_t > 0).astype(F32)
    sides = jnp.concatenate([after[0:4], before[4:8], jnp.zeros((8, mels), F32)], axis=0).astype(BF16)
    side = iota((16, RIM), 0)
    place = iota((16, RIM), 1) == jnp.where(side < 4, side, jnp.where(side < 8, side + RIM - 8, -1))
    halo[0:8] = jnp.zeros((8, RIM), F32)
    halo[mels : mels + 8] = jnp.zeros((8, RIM), F32)
    halo[4 : mels + 4] = dot(sides, place.astype(BF16), ((0,), (0,)))
    rim = halo[pl.ds(pl.multiple_of(me_m * rows, 8), BAND), :]
    near = jnp.concatenate([jnp.concatenate([above, own, below], axis=0), rim], axis=1)
    x3[...] = jnp.concatenate(
        [
            pltpu.roll(near, 1, 1) * behind,
            near,
            pltpu.roll(near, wide - 1, 1) * ahead,
            jnp.broadcast_to(usable, (BAND, wide)),
            jnp.zeros((128 - 4 * BAND, wide), F32),
        ],
        axis=0,
    ).astype(BF16)
    pre_one[...] = dot(w1[...], x3[...])
    lane = iota((1, 128), 1)
    parts = jnp.where(lane < 92, every(SUMS) + every(SUMS + 1) + every(SUMS + 2), 0.0)
    centres, numbers = parts[:, 90:91], parts[:, 91:92]
    centre = jnp.sum(centres * numbers, axis=0, keepdims=True)
    centre = centre / jnp.maximum(jnp.sum(numbers, axis=0, keepdims=True), 1.0)
    delta = centres - centre
    features = jnp.sum(parts + delta * numbers * jnp.where(lane < 81, delta, 1.0), axis=0, keepdims=True)
    moved = jnp.sum(delta * parts, axis=0, keepdims=True)
    def edge_row(k, n):
        first = FIRST * k * count + n
        return jnp.concatenate(
            [got[pl.ds(first, count, stride=FIRST), :], got[pl.ds(first + 8, count, stride=FIRST), :]], axis=1
        )

    edge_rows = [[edge_row(k, n) for n in (0, 1, 6, 7)] for k in range(n_mel)]
    zero = jnp.zeros((count, frame_dev), F32)
    rows_of = [[], [], []]
    for k, (top, second, fore, bottom) in enumerate(edge_rows):
        for n, v in enumerate((edge_rows[k - 1][3] if k else zero, top, second)):
            rows_of[n].append(v)
        for n, v in enumerate((fore, bottom, edge_rows[k + 1][0] if k + 1 < n_mel else zero)):
            rows_of[n].append(v)
    f_usable, f_behind, f_ahead = (all_masks[n * count : (n + 1) * count, :] for n in range(3))
    lane = iota((count, frame_dev), 1)

    def frame_before(v):
        v = pltpu.roll(v, 1, 1)
        return jnp.where(lane == 0, pltpu.roll(v, 1, 0), v) * f_behind

    def frame_after(v):
        v = pltpu.roll(v, frame_dev - 1, 1)
        return jnp.where(lane == frame_dev - 1, pltpu.roll(v, count - 1, 0), v) * f_ahead

    taps = []
    for group in rows_of:
        for move in (frame_before, lambda v: v, frame_after):
            taps.append(jnp.concatenate([move(v) for v in group], axis=1))
    f_usable = jnp.concatenate([f_usable] * (2 * n_mel), axis=1)
    borders = (taps, f_usable)
    edge = strips[...]
    q_usable, q_behind, q_ahead = (edge_masks[:, n : n + 1] for n in range(3))
    lane = iota((count * 8, 128), 1)
    inside = (lane < mels) & (lane % rows != 0) & (lane % rows != rows - 1)
    shifted = [
        pltpu.roll(edge, 1, 0) * q_behind,
        edge,
        pltpu.roll(edge, count * 8 - 1, 0) * q_ahead,
    ]
    taps = [pltpu.roll(v, (1 - i) % 128, 1) if i != 1 else v for i in range(3) for v in shifted]
    features = features + feature_rows(centre, borders, (taps, jnp.where(inside, q_usable, 0.0)))
    features = jnp.where(iota((1, 128), 1) < 90, features, 0.0)
    near_mean = jnp.sum(singles[...] * features, axis=1, keepdims=True) / total
    around = jnp.sum(singles[...], axis=1, keepdims=True)
    square = jnp.sum(pairs[...] * features, axis=1, keepdims=True)
    square = (square + 2.0 * around * jnp.sum(singles[...] * moved, axis=1, keepdims=True)) / total
    inv = lax.rsqrt(square - near_mean * near_mean + 1e-05)
    mean = near_mean + centre * around
    lane = iota((chan, 128), 1)
    stats[0:chan] = jnp.where(lane == 0, mean, jnp.where(lane == 1, inv, 0.0))
    stats[chan : chan + 8] = jnp.broadcast_to(to_lanes(near_mean), (8, 128))
    stats[chan + 8 : chan + 16] = jnp.broadcast_to(to_lanes(inv), (8, 128))
    scale = 0.5 * to_column(params[0:1], chan) * inv
    shift = 0.5 * to_column(params[1:2], chan) - mean * scale
    stats[chan + 16 :] = jnp.where(lane == 0, scale, jnp.where(lane == 1, shift, 0.0))
    scale = jnp.broadcast_to(scale, (chan, wide))
    shift = jnp.broadcast_to(shift, (chan, wide))
    ext = w1.shape[0] // chan
    block, taps = wf.shape
    first = jnp.zeros((chan, 128), F32)
    second = jnp.zeros((chan, 128), F32)
    own_mask = usable[:, :frame_dev]
    low_masks = [m.astype(BF16) for m in (usable, behind, ahead)]
    for r in range(ext):
        value, _ = silu_halves(pre_one[r * chan : (r + 1) * chan, :] * scale + shift)
        if not 0 <= r - 3 < rows:
            value = value * row_valid(r - 3, rows)
        base = r * 3 * chan
        low = value.astype(BF16) * low_masks[0]
        act[base : base + chan, :], act[base + 2 * chan : base + 3 * chan, :] = shifted_frames(low, *low_masks[1:])
        act[base + chan : base + 2 * chan, :] = low
        if r < 3 or r % 2 == 0:
            continue
        g = (r - 3) // 2
        result = dot(wf[...], act[g * 3 * block : g * 3 * block + taps, :frame_dev])
        pre_two[g * block : (g + 1) * block, :frame_dev] = result
        if g % 2:
            beside = [act[n * 3 * block : n * 3 * block + taps, frame_dev:] for n in (g - 1, g)]
            beside = dot(wf[...], jnp.concatenate(beside, axis=1))
            for n in range(2):
                pre_two[(g - 1 + n) * block : (g + n) * block, frame_dev:] = beside[:, n * RIM : (n + 1) * RIM]
        for q in range(2):
            if 2 <= 2 * g + q < rows + 2:
                p = result[q * chan : (q + 1) * chan]
                masked = p * own_mask
                first = first + halves(masked)
                second = second + halves(masked * p)
    moved = dot(jnp.broadcast_to(moved, (8, 128)), twice[...], precision=EXACT)[0:1]
    features_out[...] = jnp.concatenate(
        [features + moved, jnp.broadcast_to(centre, (1, 128)), jnp.zeros((6, 128), F32)], axis=0
    )
    share = share_of(devices, chan)

    def put(n, value):
        rows_out[pl.ds(n, devices, stride=SECOND), :] = jnp.broadcast_to(value, (devices, 128))

    for n in range(share):
        put(3 + n, moved_rows(every(EDGES + share + n), count))
        put(3 + share + n, moved_rows(every(EDGES + n), -count))
    for n in [0, 1, 2] + list(range(3 + 2 * share, SECOND - 1)):
        put(n, jnp.zeros((1, 128), F32))
    lane = iota((devices, 128), 1)
    tm = iota((devices, 128), 0) % count
    lefts = jnp.where(lane >= SIDE, every(SUMS), 0.0)
    rights = jnp.where(lane >= SIDE, every(SUMS + 1), 0.0)
    beside = jnp.zeros((devices, 128), F32)
    for n, step in enumerate((0, count, -count)):
        one = jnp.where(tm > 0, moved_rows(rights, step + 1), 0.0)
        two = jnp.where(tm < count - 1, moved_rows(lefts, step - 1), 0.0)
        beside = beside + pltpu.roll(one, (32 * n - SIDE) % 128, 1) + pltpu.roll(two, (32 * n + 16 - SIDE) % 128, 1)
    put(SECOND - 1, beside)
    first = jnp.sum(first, axis=1, keepdims=True)
    second = jnp.sum(second, axis=1, keepdims=True)
    parts = list(three_parts(to_lanes(first) + to_lanes(second, chan)))
    parts = jnp.concatenate(parts + [jnp.zeros((SECOND - 3, 128), F32)], axis=0)
    for d in range(devices):
        payload[d] = (rows_out[SECOND * d : SECOND * (d + 1), :] + parts).astype(BF16)


def half_share(devices, taps):
    return -(-taps // 2 // devices)


def backward_scaled(recv, pre_two, act, own_rows, params, masks,
                    grad, kept_half, sent_half, totals, pairs, stats, sides, up, right, got, beyond, halved):
    devices = recv.shape[0]
    got[...] = recv[...].astype(F32).reshape(devices * SECOND, 128)
    chan = params.shape[1]
    half = own_rows.shape[1]
    lane = iota((half, 2 * half), 1)
    spread = jnp.where(lane >> 1 == iota((half, 2 * half), 0), 0.25, 0.0).astype(BF16)
    rows = MEL_ROWS
    wide = pre_two.shape[1]
    frame_dev = wide - RIM
    usable = masks[0:1]
    share = share_of(devices, chan)
    holders = chan // share

    def every(n):
        return got[pl.ds(n, devices, stride=SECOND), :]

    beside = every(SECOND - 1)[:holders]
    lane = iota((holders, RIM), 1)
    many = rows // 2
    up[0 : many * chan] = dot(own_rows[...], spread)
    for n in range(share):
        first = n * holders
        beyond[first : first + holders, :] = every(3 + n)[:holders]
        beyond[chan + first : chan + first + holders, :] = every(3 + share + n)[:holders]
        for r in range(many + 2):
            at = many * n + (r if r < many else 32 + many - 1 if r == many else 64)
            left, right_of = beside[:, at : at + 1], beside[:, at + 16 : at + 17]
            side = jnp.where(lane >= RIM - 2, 0.25 * left, jnp.where(lane < 2, 0.25 * right_of, 0.0))
            sides[r * chan + first : r * chan + first + holders, :] = side
    up[many * chan :] = dot(beyond[...].astype(BF16), spread)
    total = masks[3:4, 0:1]
    sums = jnp.sum(every(0) + every(1) + every(2), axis=0, keepdims=True)
    mean = to_column(sums, chan) / total
    inv = lax.rsqrt(to_column(sums, chan, chan) / total - mean * mean + 1e-05)
    lane = iota((chan, 128), 1)
    scale = 0.5 * to_column(params[2:3], chan) * inv
    shift = 0.5 * to_column(params[3:4], chan) - mean * scale
    columns = jnp.zeros((chan, 128), F32)
    for n, column in enumerate((mean, inv, scale, shift)):
        columns = jnp.where(lane == n, column, columns)
    stats[0:chan] = columns
    stats[chan : chan + 8] = jnp.broadcast_to(to_lanes(inv), (8, 128))
    shift = jnp.broadcast_to(shift, (chan, wide))
    scale = jnp.broadcast_to(scale, (chan, wide))
    mean = jnp.broadcast_to(mean, (chan, frame_dev))
    inv = jnp.broadcast_to(inv, (chan, frame_dev))
    first = jnp.zeros((chan, 128), F32)
    second = jnp.zeros((chan, 128), F32)
    own_mask = usable[:, :frame_dev]
    right[3 * chan :] = jnp.ones((16, rows * frame_dev), BF16)
    table = jnp.zeros((9 * chan, 3 * chan + 16), F32)
    for q in list(range(2, rows + 2)) + [0, 1, rows + 2, rows + 3]:
        r = q // 2
        at = slice(q * chan, (q + 1) * chan)
        m = q - 2
        mask = 0.5 * usable if 0 <= m < rows else usable * (0.5 * row_valid(m, rows))
        if q % 2 == 0:
            spot = (r - 1 if 1 <= r <= many else many + (r > 0)) * chan
            upstream = jnp.concatenate([up[spot : spot + chan, :], sides[spot : spot + chan, :]], axis=1)
        pre = pre_two[at, :]
        value, slope = silu_halves(pre * scale + shift)
        g = upstream * slope * mask
        grad[at, :] = g
        if not 0 <= m < rows:
            continue
        g = g[:, :frame_dev]
        normed = (pre[:, :frame_dev] - mean) * inv
        first = first + halves(g * normed)
        second = second + halves(g)
        value = value[:, :frame_dev] * own_mask
        both = value if m % 2 == 0 else both + value
        if m % 2:
            pairs[(r - 1) * chan : r * chan, :] = both
        lanes = slice(m * frame_dev, (m + 1) * frame_dev)
        right[0:chan, lanes] = g.astype(BF16)
        right[chan : 2 * chan, lanes] = normed.astype(BF16)
        right[2 * chan : 3 * chan, lanes] = (g - right[0:chan, lanes].astype(F32)).astype(BF16)
        if m in (3, 9, rows - 1):
            start = {3: 0, 9: 4}.get(m, 10)
            left = [act[(n + 2) * 3 * chan : (n + 5) * 3 * chan, :frame_dev] for n in range(start, m + 1)]
            lanes = slice(start * frame_dev, (m + 1) * frame_dev)
            table = table + dot(jnp.concatenate(left, axis=1), right[:, lanes], ((1,), (1,)))
    first = jnp.sum(first, axis=1, keepdims=True)
    second = jnp.sum(second, axis=1, keepdims=True)
    totals[...] = jnp.broadcast_to(to_lanes(first) + to_lanes(second, chan), (8, 128))
    rest = jnp.concatenate([table[:, 2 * chan :], jnp.zeros((9 * chan, chan - 16), F32)], axis=1)
    both = table[:, : 2 * chan] + jnp.where(iota(rest.shape, 1) < chan, rest, 0.0)
    single = rest[:, chan : chan + 1]
    taps = 9 * chan // 2
    lane = iota((devices, 128), 1)
    for h in range(2):
        halved[h, 0:taps] = both[h * taps : (h + 1) * taps]
        constants = jnp.zeros((devices, 128), F32)
        for k in range(half_share(devices, 9 * chan)):
            at = h * taps + k * devices
            ones = single[at : min(at + devices, (h + 1) * taps)]
            if ones.shape[0] < devices:
                ones = jnp.concatenate([ones, jnp.zeros((devices - ones.shape[0], 1), F32)], axis=0)
            constants = jnp.where(lane == k, ones, constants)
        halved[h, taps:] = constants
    core = lax.axis_index("tm") % 2
    kept_half[...] = halved[core]
    sent_half[...] = halved[1 - core]


def pack_sums(kept_half, received, totals, payload):
    devices = kept_half.shape[0] - TAPS // 2
    block = payload.shape[0] // devices
    payload[pl.ds(0, devices, stride=block), :] = jnp.broadcast_to(totals[0:1], (devices, 128))
    taps = TAPS // 2
    total = kept_half[...] + received[...]
    for k in range(block - 2):
        cut = total[k * devices : min((k + 1) * devices, taps)]
        if cut.shape[0] < devices:
            cut = jnp.concatenate([cut, jnp.zeros((devices - cut.shape[0], 128), F32)], axis=0)
        payload[pl.ds(1 + k, devices, stride=block), :] = cut
    payload[pl.ds(block - 1, devices, stride=block), :] = total[taps:]


def pool(totals, pairs, out, gain_out, bias_out, temp):
    gain_out[...] = totals[0:1, : gain_out.shape[1]]
    bias_out[...] = totals[0:1, gain_out.shape[1] :]
    chan, rows, half = out.shape[1:]
    to_mean = jnp.where(iota((2 * half, half), 0) >> 1 == iota((2 * half, half), 1), 0.25, 0.0)
    pooled = dot(pairs[...], to_mean, precision=EXACT)
    for r in range(rows):
        temp[pl.ds(r, chan, stride=rows), :] = pooled[r * chan : (r + 1) * chan]
    out[0] = temp[...].reshape(chan, rows, half).astype(BF16)


def backward(recv, pre_two, grad, stats_two, w1, x3, stats, params, masks, wb,
             out, own_low, payload, totals, g3, pre_one, g1):
    chan = params.shape[1]
    rows = MEL_ROWS
    wide = pre_two.shape[1]
    frame_dev = wide - RIM
    usable = masks[0:1]
    behind, ahead = (masks[n : n + 1].astype(BF16) for n in (1, 2))
    total = masks[3:4, 0:1]
    devices = payload.shape[0] // 14
    pre_one[...] = dot(w1[3 * chan : (rows + 3) * chan], x3[:, :frame_dev])

    even, odd = summed_blocks(recv, devices, 2)
    sums = even[0:1] + odd[0:1]
    gain_sum, bias_sum = sums[:, :chan], sums[:, chan:]
    totals[...] = jnp.broadcast_to(sums, (8, 128))
    mean, inv = stats_two[0:chan, 0:1], stats_two[0:chan, 1:2]
    factor = to_column(params[2:3], chan) * inv
    gain_part = factor * (to_column(sums, chan) / total * inv)
    bias_part = factor * (to_column(sums, chan, chan) / total) - mean * gain_part
    gain_part = jnp.broadcast_to(gain_part, (chan, wide))
    bias_part = jnp.broadcast_to(bias_part, (chan, wide))
    factor = jnp.broadcast_to(factor, (chan, wide))
    scale = jnp.broadcast_to(stats[chan + 16 :, 0:1], (chan, frame_dev))
    shift = jnp.broadcast_to(stats[chan + 16 :, 1:2], (chan, frame_dev))
    factor_one = jnp.broadcast_to(to_column(params[0:1], chan) * stats[0:chan, 1:2], (chan, frame_dev))
    own_mask = 0.5 * usable[:, :frame_dev]
    count = pre_two.shape[0] // chan
    table = jnp.zeros((chan, 128), F32)

    def tap_sums(m):
        part = g1[m * chan : (m + 4) * chan, :]
        high = lax.reduce_precision(part, 8, 7)
        low = (part - high).astype(BF16)
        taps_in = x3[:, :frame_dev]
        products = dot(high.astype(BF16), taps_in, ((1,), (1,))) + dot(low, taps_in, ((1,), (1,)))
        moved = [pltpu.roll(products[k * chan : (k + 1) * chan], 128 - (m + k + 3), 1) for k in range(4)]
        return (moved[0] + moved[1]) + (moved[2] + moved[3])

    for q in range(count):
        at = slice(q * chan, (q + 1) * chan)
        mask = usable if 0 <= q - 2 < rows else usable * row_valid(q - 2, rows)
        low = (factor * grad[at, :] - (bias_part + pre_two[at, :] * gain_part) * mask).astype(BF16)
        out[at, :] = low
        if not 1 <= q < count - 1:
            continue
        base = (q - 1) * 3 * chan
        for n, v in enumerate((low,) + shifted_frames(low, behind, ahead)):
            spot = base + (1, 0, 2)[n] * chan
            g3[spot : spot + chan, :] = v[:, :frame_dev]
        start = q - 4
        if start < 0 or start % 2:
            continue
        result = dot(wb[...], g3[start * 3 * chan : (start + 4) * 3 * chan, :])
        for n in range(2):
            m = start + n
            at = slice(m * chan, (m + 1) * chan)
            _, slope = silu_halves(pre_one[at, :] * scale + shift)
            value = result[n * chan : (n + 1) * chan] * slope * own_mask
            own_low[at, :] = (value * factor_one).astype(BF16)
            g1[at, :] = value
        if start % 4 == 2 and start > 2:
            table = table + tap_sums(start - 6)
    table = table + tap_sums(rows - 4)
    table = table.T
    places = [BAND * j + i for i in range(3) for j in range(3)] + [3 * BAND]
    rows10 = jnp.concatenate([table[n : n + 1] for n in places], axis=0)
    share = even.shape[0] - 2
    mine = jnp.concatenate([even[1 : share + 1], odd[1 : share + 1]], axis=0)
    single = jnp.concatenate([to_column(v[share + 1 :], share) for v in (even, odd)], axis=0)
    factor_l = params[2:3] * stats_two[chan : chan + 1, :chan]
    mine = mine[:, :chan] - (bias_sum * single + gain_sum * mine[:, chan:]) / total
    mine = factor_l * mine
    mine = jnp.concatenate([mine[:share], mine[share:]], axis=1)
    if share < 9:
        mine = jnp.concatenate([mine, jnp.zeros((9 - share, 128), F32)], axis=0)
    sums = jnp.concatenate([rows10[0:5], rows10[5:10]], axis=1)
    block = jnp.concatenate([sums, mine], axis=0)
    block = jnp.concatenate([block] * 4, axis=0)
    for d in range(0, devices, 4):
        payload[14 * d : 14 * (d + 4), :] = block


def transposed(grad, own_low, w1, wb, x3, stats, features, k1t, params, masks, ws_hbm,
               first, ws, normed_taps, low, g3, rim, sem):
    load = pltpu.make_async_copy(ws_hbm, ws, sem)
    load.start()
    rows = MEL_ROWS
    chan = own_low.shape[0] // rows
    wide = grad.shape[1]
    frame_dev = wide - RIM
    count = grad.shape[0] // chan
    usable = masks[0:1]
    behind, ahead = (masks[n : n + 1].astype(BF16) for n in (1, 2))
    scale = jnp.broadcast_to(stats[chan + 16 :, 0:1], (chan, wide))
    shift = jnp.broadcast_to(stats[chan + 16 :, 1:2], (chan, wide))
    factor = jnp.broadcast_to(to_column(params[0:1], chan) * stats[0:chan, 1:2], (chan, wide))
    edge = (0, 1, 2, 3, count - 4, count - 3, count - 2, count - 1)
    for q in range(count):
        value = grad[q * chan : (q + 1) * chan, :]
        for n, v in enumerate((value,) + shifted_frames(value, behind, ahead)):
            spot = (3 * q + (1, 0, 2)[n]) * chan
            rim[spot : spot + chan, :] = v[:, frame_dev:]
            if q in edge:
                spot = (3 * edge.index(q) + (1, 0, 2)[n]) * chan
                g3[spot : spot + chan, :] = v[:, :frame_dev]
    low[chan : (rows + 1) * chan, :frame_dev] = own_low[...]

    def put(m, lanes, result, pre_one):
        at = slice((m + 1) * chan, (m + 2) * chan)
        _, slope = silu_halves(pre_one * scale[:, lanes] + shift[:, lanes])
        mask = usable[:, lanes] * (0.5 * row_valid(m, rows))
        low[at, lanes] = (result * slope * mask * factor[:, lanes]).astype(BF16)

    pre_one = dot(w1[2 * chan : (rows + 4) * chan, :], x3[:, frame_dev:])
    beside = slice(frame_dev, wide)
    for start in range(0, rows + 2, 2):
        result = dot(wb[...], rim[start * 3 * chan : (start + 4) * 3 * chan, :])
        for n in range(2):
            at = slice((start + n) * chan, (start + n + 1) * chan)
            put(start + n - 1, beside, result[n * chan : (n + 1) * chan], pre_one[at])
    own = slice(0, frame_dev)
    result = dot(wb[...], g3[: 4 * 3 * chan, :])
    put(-1, own, result[:chan], dot(w1[2 * chan : 3 * chan, :], x3[:, :frame_dev]))
    result = dot(wb[...], g3[4 * 3 * chan :, :])
    put(rows, own, result[chan:], dot(w1[(rows + 3) * chan : (rows + 4) * chan, :], x3[:, :frame_dev]))
    row = features[0:1, :]
    lane = iota((1, 128), 1)
    gram = jnp.concatenate(
        [jnp.where(lane < 9, pltpu.roll(row, 128 - 9 * t, 1) if t else row, 0.0) for t in range(9)]
        + [jnp.zeros((7, 128), F32)],
        axis=0,
    )
    single = to_column(row, 16, 81)[0:9]
    k_rows = jnp.concatenate([k1t[...], jnp.zeros((112, chan), F32)], axis=0)
    mean_l, inv_l = stats[chan : chan + 1, :chan], stats[chan + 8 : chan + 9, :chan]
    normed = inv_l * (dot(gram, k_rows, precision=EXACT)[0:9] - single * mean_l)
    normed_taps[0:16] = jnp.concatenate([normed, jnp.zeros((7, chan), F32)], axis=0)
    normed_taps[16:32] = jnp.broadcast_to(to_column(row, 16, 81), (16, chan))
    load.wait()
    first[...] = dot(ws[...], low[...])


def finish(recv, features, stats, k1t, first, ws, w1, x3, normed_taps, params, masks,
           spec_hbm, kernel_one_hbm, kernel_two_hbm, gain_hbm, bias_hbm,
           spec_grad, kernel_one, kernel_two, gain_out, bias_out, sems):
    chan = params.shape[1]
    rows = MEL_ROWS
    wide = x3.shape[1]
    frame_dev = wide - RIM
    usable, behind, ahead = (masks[n : n + 1] for n in range(3))
    total = masks[3:4, 0:1]
    gain = params[0:1]
    count = recv.shape[0] // 14
    share = half_share(count, 9 * chan)
    left = [recv[pl.ds(5 + p, count, stride=14), :] for p in range(share)]
    taps = TAPS // 2
    whole = [jnp.concatenate([v[:, h * chan : (h + 1) * chan] for v in left], axis=0)[:taps] for h in range(2)]
    whole = jnp.concatenate(whole, axis=0)
    for t in range(9):
        kernel_two[t] = whole[t * chan : (t + 1) * chan].T
    stores = [pltpu.make_async_copy(kernel_two, kernel_two_hbm, sems.at[4])]
    stores[0].start()
    sums = summed_blocks(recv, count)[0:5]
    ten = jnp.concatenate([sums[:, :chan], sums[:, chan:]], axis=0)
    bias_sum = ten[9:10]
    mean_l, inv_l = stats[chan : chan + 1, :chan], stats[chan + 8 : chan + 9, :chan]
    ten = ten - features[1:2, 0:1] * bias_sum
    k = k1t[0:9]
    gain_sum = inv_l * (jnp.sum(k * ten[0:9], axis=0, keepdims=True) - mean_l * bias_sum)
    gain_out[...] = gain_sum
    bias_out[...] = bias_sum
    factor_l = gain * inv_l
    scale = factor_l * gain_sum / total * inv_l
    scale = jnp.concatenate(
        [scale * row_valid(-1, rows)] + [scale] * rows + [scale * row_valid(rows, rows)], axis=1
    )
    many = 3 * rows

    def in_parts(v, right):
        high = lax.reduce_precision(v, 8, 7)
        v = dot(jnp.concatenate([high, v - high], axis=0).astype(BF16), right)
        return v[:many] + v[many:]

    taken = in_parts(in_parts(ws[...].astype(F32) * scale, w1[2 * chan : (rows + 4) * chan, :]), x3[...])
    taps = first[...] - taken
    moved = [taps[rows * b : rows * (b + 1)] for b in range(3)]
    mean_full = mean_l + features[1:2, 0:1] * jnp.sum(k, axis=0, keepdims=True)
    constant = jnp.sum(k * (factor_l * (bias_sum - gain_sum * inv_l * mean_full) / total), axis=1, keepdims=True)
    for a in range(3):
        row = iota((rows, 1), 0) + (a - 1) + lax.axis_index("mel") * rows
        valid = ((row >= 0) & (row < lax.axis_size("mel") * rows)).astype(F32) * usable
        for b in range(3):
            t = 3 * (2 - a) + 2 - b
            moved[b] = moved[b] - constant[t : t + 1] * valid
    result = pltpu.roll(moved[0], 1, 1) * behind + moved[1] + pltpu.roll(moved[2], wide - 1, 1) * ahead
    spec_grad[0] = (result * usable)[:, :frame_dev]
    grad_taps = factor_l * (ten[0:9] - (bias_sum * normed_taps[16:25] + gain_sum * normed_taps[0:9]) / total)
    for i in range(3):
        kernel_one[i] = grad_taps[3 * i : 3 * i + 3]
    outs = ((spec_grad, spec_hbm), (kernel_one, kernel_one_hbm), (gain_out, gain_hbm), (bias_out, bias_hbm))
    wait_all(stores + start_all(*outs, sems=sems))


def run(kernel, outs, scratch, *args, hbm=0, apart=(), flops=10**8, size=4 * 10**6):
    vmem = pl.BlockSpec(memory_space=pltpu.VMEM)
    devices = lax.axis_size("mel") * lax.axis_size("tm")
    specs = []
    args = list(args)
    for n, a in enumerate(args):
        if hbm and n >= len(args) - hbm:
            specs.append(pl.BlockSpec(memory_space=pltpu.HBM))
            args[n] = pltpu.with_memory_space_constraint(a, pltpu.HBM)
        else:
            specs.append(vmem)
            args[n] = pltpu.with_memory_space_constraint(a, pltpu.VMEM)
    return pl.pallas_call(
        kernel,
        out_shape=outs,
        in_specs=specs,
        out_specs=[pl.BlockSpec(memory_space=pltpu.HBM) if n in apart else vmem for n in range(len(outs))],
        scratch_shapes=scratch,
        compiler_params=pltpu.CompilerParams(vmem_limit_bytes=(29 + devices // 32) * 2**20),
        cost_estimate=pl.CostEstimate(flops=flops, bytes_accessed=size, transcendentals=0),
    )(*args)


def shape(dims, dtype=F32):
    return jax.ShapeDtypeStruct(dims, dtype)


def kept(dims, dtype=F32):
    return pltpu.VMEM(dims, dtype)


def far(dims, dtype=F32):
    return pltpu.HBM(dims, dtype)


def exchange(blocks, axes=AXES):
    return lax.all_to_all(blocks, axes, 0, 0, tiled=True)


def exchange_rows(rows, axes=AXES):
    return exchange(rows[:, None, :], axes)[:, 0, :]


def shards(spectrum, clip_bounds, kernel_one, gain_one, bias_one, kernel_two, gain_two, bias_two, pooled_grad):
    _, rows, frame_dev = spectrum.shape
    chan = kernel_two.shape[0]
    n_mel, n_tm = lax.axis_size("mel"), lax.axis_size("tm")
    devices = n_mel * n_tm
    half = frame_dev // 2
    wide = frame_dev + RIM
    mels = n_mel * rows

    packed, own, spec, masks = run(
        pack,
        [
            kept((devices, FIRST, 128), BF16),
            kept(pooled_grad.shape, BF16),
            kept(spectrum.shape, BF16),
            kept((8, wide)),
        ],
        [
            pltpu.SMEM(clip_bounds.shape, jnp.int32),
            pltpu.VMEM((2 * chan, half), F32),
            pltpu.VMEM((devices * FIRST, 128), F32),
            pltpu.SemaphoreType.DMA((3,)),
        ],
        spectrum,
        pooled_grad,
        clip_bounds,
        hbm=3,
    )
    recv = exchange(packed)
    ext = rows + 6
    span = 4 * 3 * chan
    wf, wb, w1, ws, pairs, singles, k1t, params, all_masks, edge_masks, twice, own_rows = run(
        weights,
        [
            kept((2 * chan, span), BF16),
            kept((2 * chan, span), BF16),
            kept((ext * chan, 128), BF16),
            far((rows * 3, (rows + 2) * chan), BF16),
            kept((chan, 128)),
            kept((chan, 128)),
            kept((16, chan)),
            kept((8, chan)),
            kept((3 * n_tm, frame_dev)),
            kept((n_tm * 8, 128)),
            kept((128, 128)),
            kept((chan * rows // 2, half), BF16),
        ],
        [
            pltpu.VMEM((9, chan, chan), BF16),
            pltpu.VMEM((3, 3, chan), BF16),
            pltpu.VMEM((4, 1, chan), F32),
            pltpu.SMEM(clip_bounds.shape, jnp.int32),
            pltpu.VMEM((rows * 3, (rows + 2) * chan), BF16),
            pltpu.VMEM((chan * rows // 2, half), F32),
            pltpu.SemaphoreType.DMA((8,)),
        ],
        own,
        clip_bounds,
        jnp.transpose(kernel_two, (2, 3, 0, 1)).reshape(9, chan, chan),
        jnp.transpose(kernel_one, (1, 2, 0)),
        gain_one[None],
        bias_one[None],
        gain_two[None],
        bias_two[None],
        hbm=7,
        apart=(3,),
    )
    pre_two, payload, act, x3, stats_one, features = run(
        forward_one,
        [
            kept(((rows + 4) * chan, wide)),
            kept((devices, SECOND, 128), BF16),
            kept((ext * 3 * chan, wide), BF16),
            kept((128, wide), BF16),
            kept((2 * chan + 16, 128)),
            kept((8, 128)),
        ],
        [
            pltpu.VMEM((ext * chan, wide), F32),
            pltpu.VMEM((devices * FIRST, 128), F32),
            pltpu.VMEM((n_tm * 8, 128), F32),
            pltpu.VMEM((mels + 8, RIM), F32),
            pltpu.VMEM((devices * SECOND, 128), F32),
        ],
        recv,
        spec,
        pairs,
        singles,
        twice,
        w1,
        wf,
        params,
        masks,
        all_masks,
        edge_masks,
    )
    recv = exchange(payload)
    grad, kept_half, sent_half, totals, row_pairs, stats_two = run(
        backward_scaled,
        [
            kept(((rows + 4) * chan, wide)),
            kept((TAPS // 2 + devices, 128)),
            kept((TAPS // 2 + devices, 128)),
            kept((8, 128)),
            kept((rows // 2 * chan, frame_dev)),
            kept((chan + 8, 128)),
        ],
        [
            pltpu.VMEM(((rows // 2 + 2) * chan, RIM), F32),
            pltpu.VMEM(((rows // 2 + 2) * chan, frame_dev), F32),
            pltpu.VMEM((3 * chan + 16, rows * frame_dev), BF16),
            pltpu.VMEM((devices * SECOND, 128), F32),
            pltpu.VMEM((2 * chan, half), F32),
            pltpu.VMEM((2, TAPS // 2 + devices, 128), F32),
        ],
        recv,
        pre_two,
        act,
        own_rows,
        params,
        masks,
    )
    received = lax.ppermute(sent_half, "tm", [(i, i ^ 1) for i in range(n_tm)])
    (payload,) = run(
        pack_sums,
        [kept((devices * (half_share(devices, 9 * chan) + 2), 128))],
        [],
        kept_half,
        received,
        totals,
    )
    recv = exchange_rows(payload)
    grad, own_low, payload, totals = run(
        backward,
        [
            kept(((rows + 4) * chan, wide), BF16),
            kept((rows * chan, frame_dev), BF16),
            kept((devices * 14, 128)),
            kept((8, 128)),
        ],
        [
            pltpu.VMEM(((rows + 2) * 3 * chan, frame_dev), BF16),
            pltpu.VMEM((rows * chan, frame_dev), F32),
            pltpu.VMEM((rows * chan, frame_dev), F32),
        ],
        recv,
        pre_two,
        grad,
        stats_two,
        w1,
        x3,
        stats_one,
        params,
        masks,
        wb,
    )
    recv = exchange_rows(payload)
    pooled, gain_two_grad, bias_two_grad = run(
        pool,
        [shape((1, chan, rows // 2, half), BF16), shape((1, chan)), shape((1, chan))],
        [
            pltpu.VMEM((rows // 2 * chan, 128), F32),
        ],
        totals,
        row_pairs,
    )
    first, ws, normed_taps = run(
        transposed,
        [
            kept((rows * 3, wide)),
            kept((rows * 3, (rows + 2) * chan), BF16),
            kept((32, chan)),
        ],
        [
            pltpu.VMEM(((rows + 2) * chan, wide), BF16),
            pltpu.VMEM((8 * 3 * chan, frame_dev), BF16),
            pltpu.VMEM(((rows + 4) * 3 * chan, RIM), BF16),
            pltpu.SemaphoreType.DMA,
        ],
        grad,
        own_low,
        w1,
        wb,
        x3,
        stats_one,
        features,
        k1t,
        params,
        masks,
        ws,
        hbm=1,
    )
    spec_grad, kernel_one_grad, kernel_two_grad, gain_one_grad, bias_one_grad = run(
        finish,
        [
            shape((1, rows, frame_dev)),
            shape((3, 3, chan)),
            shape((9, chan, chan)),
            shape((1, chan)),
            shape((1, chan)),
        ],
        [
            pltpu.VMEM((1, rows, frame_dev), F32),
            pltpu.VMEM((3, 3, chan), F32),
            pltpu.VMEM((9, chan, chan), F32),
            pltpu.VMEM((1, chan), F32),
            pltpu.VMEM((1, chan), F32),
            pltpu.SemaphoreType.DMA((5,)),
        ],
        recv,
        features,
        stats_one,
        k1t,
        first,
        ws,
        w1,
        x3,
        normed_taps,
        params,
        masks,
        apart=range(5),
    )
    kernel_two_grad = jnp.transpose(kernel_two_grad.reshape(3, 3, chan, chan), (2, 3, 0, 1))
    return (
        pooled,
        spec_grad,
        jnp.transpose(kernel_one_grad, (2, 0, 1)),
        gain_one_grad[0],
        bias_one_grad[0],
        kernel_two_grad,
        gain_two_grad[0],
        bias_two_grad[0],
    )


def solution(mesh):
    return jax.shard_map(
        shards,
        mesh=mesh,
        in_specs=(
            P(None, "mel", "tm"),
            P(),
            P(),
            P(),
            P(),
            P(),
            P(),
            P(),
            P(None, None, "mel", "tm"),
        ),
        out_specs=(P(None, None, "mel", "tm"), P(None, "mel", "tm"), P(), P(), P(), P(), P(), P()),
        check_vma=False,
    )
```

```python
import math

import jax
import jax.numpy as jnp
from jax import lax
from jax.experimental import pallas as pl
from jax.experimental.pallas import tpu as pltpu
from jax.sharding import PartitionSpec as P

F32 = jnp.float32
BF16 = jnp.bfloat16
AXES = ("mel", "tm")
EXACT = lax.Precision.HIGHEST
RIM = 128
BAND = 24
MEL_ROWS = 16
FIRST = 24
SUMS, EDGES, COLUMNS = 16, 19, 23
SIDE = 96
TAPS = 576
SECOND = 8


def iota(shape, dim):
    return lax.broadcasted_iota(jnp.int32, shape, dim)


def dot(a, b, over=((1,), (0,)), precision=None):
    return lax.dot_general(a, b, (over, ((), ())), precision=precision, preferred_element_type=F32)


def to_column(lanes, count, start=0):
    shape = (count, lanes.shape[1])
    return jnp.sum(jnp.where(iota(shape, 1) == iota(shape, 0) + start, lanes, 0.0), axis=1, keepdims=True)


def to_lanes(column, start=0, width=128):
    shape = (column.shape[0], width)
    return jnp.sum(jnp.where(iota(shape, 1) == iota(shape, 0) + start, column, 0.0), axis=0, keepdims=True)


def halves(v):
    total = v[:, :128]
    for n in range(128, v.shape[1], 128):
        total = total + v[:, n : n + 128]
    return total


def frame_masks(bounds, frames):
    last = bounds.shape[1] - 1

    def living(f):
        return (f >= 0) & (f < bounds[0, last])

    def paired(f):
        both = living(f) & living(f + 1)
        for k in range(1, last):
            both = both & (f + 1 != bounds[0, k])
        return both

    return tuple(m.astype(F32) for m in (living(frames), paired(frames - 1), paired(frames)))


def row_valid(row, rows):
    mel = lax.axis_index("mel") * rows + row
    return ((mel >= 0) & (mel < lax.axis_size("mel") * rows)).astype(F32)


def start_all(*pairs, sems):
    copies = [pltpu.make_async_copy(src, dst, sems.at[n]) for n, (src, dst) in enumerate(pairs)]
    for copy in copies:
        copy.start()
    return copies


def wait_all(copies):
    for copy in copies:
        copy.wait()


def shifted_frames(value, behind, ahead):
    wide = value.shape[1]
    return pltpu.roll(value, 1, 1) * behind, pltpu.roll(value, wide - 1, 1) * ahead


def three_parts(v):
    high = lax.reduce_precision(v, 8, 7)
    mid = lax.reduce_precision(v - high, 8, 7)
    return high, mid, v - high - mid


def share_of(devices, chan):
    return -(-chan // devices)


def pack(spec_hbm, grad_hbm, bounds_hbm, out, own, spec, masks, bounds, edges, rows_out, sems):
    copies = start_all((bounds_hbm, bounds), (spec_hbm, spec), (grad_hbm, own), sems=sems)
    copies[0].wait()
    wide = masks.shape[1]
    frame_dev = wide - RIM
    devices = out.shape[0]
    rows = MEL_ROWS
    lane = iota((1, wide), 1)
    frames = lax.axis_index("tm") * frame_dev + jnp.where(lane < frame_dev + RIM // 2, lane, lane - wide)
    last = bounds.shape[1] - 1
    pixels = (bounds[0, last] * (lax.axis_size("mel") * rows)).astype(F32)
    found = frame_masks(bounds, frames)
    masks[...] = jnp.concatenate(
        list(found) + [jnp.full((1, wide), 1.0) * pixels, jnp.zeros((4, wide), F32)], axis=0
    )
    usable, behind, ahead = (m[:, :frame_dev] for m in found)
    copies[1].wait()
    x = spec[0].astype(F32) * usable
    lane = iota((1, frame_dev), 1)
    row = iota((rows, 1), 0)
    inner = jnp.where((lane > 0) & (lane < frame_dev - 1), usable, 0.0)
    number = (rows - 2) * jnp.sum(inner, axis=1, keepdims=True)
    inner = inner * ((row > 0) & (row < rows - 1)).astype(F32)
    centre = jnp.sum(jnp.sum(x, axis=0, keepdims=True), axis=1, keepdims=True)
    centre = centre / (rows * jnp.maximum(jnp.sum(usable, axis=1, keepdims=True), 1.0))
    centre = lax.reduce_precision(centre, 8, 7)
    shifted = [pltpu.roll(x, 1, 1) * behind, x, pltpu.roll(x, frame_dev - 1, 1) * ahead]
    taps = [pltpu.roll(v, (1 - i) % rows, 0) if i != 1 else v for i in range(3) for v in shifted]
    features = feature_rows(centre, (taps, inner))
    lane = iota((1, 128), 1)
    features = jnp.where(lane == 90, centre, jnp.where(lane == 91, number, features))
    pick = iota((8, frame_dev), 0)
    column = jnp.where(pick < 4, pick, frame_dev - 8 + pick)
    strip = dot((iota((8, frame_dev), 1) == column).astype(BF16), x.astype(BF16), ((1,), (1,)))
    lane = iota((8, 128), 1)
    repeat = (iota((rows, 128), 1) % rows == iota((rows, 128), 0)).astype(BF16)
    strip = jnp.where(lane // rows == iota((8, 128), 0), dot(strip.astype(BF16), repeat), 0.0)
    strip = jnp.sum(strip, axis=0, keepdims=True)

    def put(n, value):
        rows_out[pl.ds(n, devices, stride=FIRST), :] = jnp.broadcast_to(value, (devices, 128))

    near = jnp.concatenate([x[0:4], x[rows - 4 :]], axis=0)
    near = jnp.concatenate([near[:, :128], near[:, 128:]], axis=0)
    for d in range(devices):
        rows_out[FIRST * d : FIRST * d + 16, :] = near
    put(COLUMNS, strip)
    copies[2].wait()
    _, chan, many, half = own.shape
    share = share_of(devices, chan)
    holders = chan // share
    g = own[0].astype(F32)
    edges[0:chan] = g[:, 0, :]
    edges[chan:] = g[:, many - 1, :]

    def spread_out(v):
        if holders < devices:
            v = jnp.concatenate([v, jnp.zeros((devices - holders, 128), F32)], axis=0)
        return v

    for n in range(share):
        put(EDGES + n, spread_out(edges[n * holders : (n + 1) * holders, :]))
        put(EDGES + share + n, spread_out(edges[chan + n * holders : chan + (n + 1) * holders, :]))
    for n in range(2 * share, COLUMNS - EDGES):
        put(EDGES + n, jnp.zeros((1, 128), F32))
    end = iota((8, half), 0)
    at = iota((8, half), 1)
    ends = ((end == 0) & (at == 0)) | ((end == 1) & (at == half - 1))
    columns = dot(ends.astype(BF16), g.reshape(chan * many, half).astype(BF16), ((1,), (1,)))
    group = 128 // many
    source = iota((128, 128), 0)
    lane = iota((group, 128), 1)
    mine = lane // many == iota((group, 128), 0)
    parts = three_parts(features)
    for n in range(2):
        side = jnp.zeros((holders, 128), F32)
        for m in range(share):
            move = (iota((128, 128), 1) == SIDE + many * m + source % many).astype(BF16)
            first = m * holders * many // 128
            block = [columns[n : n + 1, 128 * q : 128 * (q + 1)] for q in range(first, first + holders * many // 128)]
            block = jnp.concatenate([jnp.where(mine, v, 0.0) for v in block], axis=0)
            side = side + dot(block.astype(BF16), move)
        put(SUMS + n, spread_out(side) + parts[n])
    put(SUMS + 2, parts[2])
    out[...] = rows_out[...].reshape(out.shape).astype(BF16)


def weights(own, bounds_hbm, k2_hbm, k1_hbm, gain_one_hbm, bias_one_hbm, gain_two_hbm, bias_two_hbm,
            wf, wb, w1, ws_hbm, pairs, singles, k1t, params, all_masks, edge_masks, twice, own_rows,
            k2, k1, vectors, bounds, ws, temp, sems):
    loads = start_all(
        (bounds_hbm, bounds),
        (k2_hbm, k2),
        (k1_hbm, k1),
        (gain_one_hbm, vectors.at[0]),
        (bias_one_hbm, vectors.at[1]),
        (gain_two_hbm, vectors.at[2]),
        (bias_two_hbm, vectors.at[3]),
        sems=sems,
    )
    _, many, count, half = own.shape
    temp[...] = own[0].astype(F32).reshape(many * count, half)
    for r in range(count):
        own_rows[r * many : (r + 1) * many] = temp[pl.ds(r, many, stride=count), :].astype(BF16)
    wait_all(loads)
    chan = k2.shape[1]
    span = wf.shape[1]
    taps = [k2[t].astype(F32) for t in range(9)]
    rest = jnp.zeros((chan, span - 9 * chan), F32)
    forward = jnp.concatenate(taps + [rest], axis=1)
    backward = jnp.concatenate([taps[8 - t].T for t in range(9)] + [rest], axis=1)
    for r in range(wb.shape[0] // chan):
        at = slice(r * chan, (r + 1) * chan)
        wb[at] = (pltpu.roll(backward, 3 * chan * r, 1) if r else backward).astype(BF16)
    full = jnp.concatenate([k1[n].astype(F32) for n in range(3)] + [jnp.zeros((7, chan), F32)], axis=0)
    low = [
        jnp.concatenate([full[3 * (2 - a) + 2 - b : 3 * (2 - a) + 3 - b] for a in range(3)], axis=1)
        for b in range(3)
    ]
    rest = jnp.zeros((1, ws.shape[1] - 3 * chan), F32)
    for b in range(3):
        base = jnp.concatenate([low[b], rest], axis=1)
        many = ws.shape[0] // 3
        rolled = [pltpu.roll(base, chan * m, 1) if m else base for m in range(many)]
        ws[many * b : many * (b + 1)] = jnp.concatenate(rolled, axis=0).astype(BF16)
    store_ws = pltpu.make_async_copy(ws, ws_hbm, sems.at[7])
    store_ws.start()
    count, frame_dev = all_masks.shape[0] // 3, all_masks.shape[1]
    frames = iota((count, frame_dev), 0) * frame_dev + iota((count, frame_dev), 1)
    for n, mask in enumerate(frame_masks(bounds, frames)):
        all_masks[n * count : (n + 1) * count] = mask
    q = iota(edge_masks.shape, 0)
    lane = iota(edge_masks.shape, 1)
    k = q % 8
    frames = (q // 8) * frame_dev + jnp.where(k < 4, k, k + frame_dev - 8)
    living, behind, ahead = frame_masks(bounds, frames)
    living = jnp.where((k == 0) | (k == 7), living, 0.0)
    edge_masks[...] = jnp.where(lane == 0, living, jnp.where(lane == 1, behind, jnp.where(lane == 2, ahead, 0.0)))
    params[...] = jnp.concatenate(
        [vectors[n] for n in range(4)] + [jnp.zeros((4, chan), F32)], axis=0
    )
    tap = iota((16, 128), 0)
    lane = iota((16, 128), 1)
    i = (tap * 11) >> 5
    ninth = (lane * 57) >> 9
    to_band = (lane == BAND * (tap - 3 * i) + i) & (tap < 9)
    to_left = (ninth == tap) & (tap < 9)
    to_right = (lane - 9 * ninth == tap) & (lane < 81)
    to_single = (lane == 81 + tap) & (tap < 9)
    source = iota((128, 128), 0) - 81
    lane = iota((128, 128), 1)
    ninth = (lane * 57) >> 9
    inside = (source >= 0) & (source < 9) & (lane < 81)
    twice[...] = jnp.where(inside, (source == ninth).astype(F32) + (source == lane - 9 * ninth).astype(F32), 0.0)
    for r in range(wf.shape[0] // chan):
        at = slice(r * chan, (r + 1) * chan)
        wf[at] = (pltpu.roll(forward, 3 * chan * r, 1) if r else forward).astype(BF16)
    k1t[...] = full
    k = full.astype(BF16)
    lanes = [dot(k, select.astype(BF16), ((0,), (0,))) for select in (to_band, to_left, to_right, to_single)]
    pairs[...] = lanes[1] * lanes[2]
    singles[...] = lanes[3]
    for m in range(w1.shape[0] // chan):
        w1[m * chan : (m + 1) * chan] = (pltpu.roll(lanes[0], m, 1) if m else lanes[0]).astype(BF16)
    store_ws.wait()


def feature_rows(centre, *parts):
    def folded(v):
        return jnp.sum(halves(v), axis=0, keepdims=True)

    rows = [jnp.zeros((1, 128), F32)] * 96
    for taps, weight in parts:
        z = [tap - centre for tap in taps]
        for s in range(9):
            left = z[s] * weight
            rows[81 + s] = rows[81 + s] + folded(left)
            for t in range(s, 9):
                rows[9 * s + t] = rows[9 * t + s] = rows[9 * s + t] + folded(left * z[t])
    return to_lanes(jnp.sum(jnp.concatenate(rows, axis=0), axis=1, keepdims=True))


def summed_blocks(ref, devices, by=1):
    block = ref.shape[0] // devices
    period = max(8 // math.gcd(block, 8), by)
    step = period * block
    total = ref[0:step, :]
    for at in range(step, ref.shape[0], step):
        total = total + ref[at : at + step, :]
    results = []
    for first in range(by):
        result = total[first * block : (first + 1) * block]
        for n in range(first + by, period, by):
            result = result + total[n * block : (n + 1) * block]
        results.append(result)
    return results if by > 1 else results[0]


def moved_rows(v, step):
    if step == 0:
        return v
    count = v.shape[0]
    if abs(step) >= count:
        return jnp.zeros_like(v)
    zero = jnp.zeros((abs(step), v.shape[1]), v.dtype)
    if step > 0:
        return jnp.concatenate([zero, v[: count - step]], axis=0)
    return jnp.concatenate([v[-step:], zero], axis=0)


def silu_halves(h):
    t = jnp.tanh(h)
    one = 1.0 + t
    return h * one, one * (1.0 + h * (1.0 - t))


def forward_one(recv, spec, pairs, singles, twice, w1, wf, params, masks, all_masks, edge_masks,
                pre_two, payload, act, x3, stats, features_out, pre_one, got, strips, halo, rows_out):
    devices = recv.shape[0]
    n_mel, count = lax.axis_size("mel"), lax.axis_size("tm")
    rows = MEL_ROWS
    mels = n_mel * rows
    wide = masks.shape[1]
    frame_dev = wide - RIM
    chan = params.shape[1]
    me_m, me_t = lax.axis_index("mel"), lax.axis_index("tm")
    usable, behind, ahead = (masks[n : n + 1] for n in range(3))
    total = masks[3:4, 0:1]
    got[...] = recv[...].astype(F32).reshape(devices * FIRST, 128)

    def every(n):
        return got[pl.ds(n, devices, stride=FIRST), :]

    lane = iota((count, 128), 1)
    bands = [got[pl.ds(FIRST * k * count + COLUMNS, count, stride=FIRST), :] for k in range(n_mel)]
    for c in range(8):
        column = jnp.zeros((count, 128), F32)
        for k, band in enumerate(bands):
            part = jnp.where(lane // rows == c, band, 0.0)
            column = column + (pltpu.roll(part, rows * (k - c) % 128, 1) if k != c else part)
        strips[pl.ds(c, count, stride=8), :] = column
    at = pl.multiple_of(FIRST * (jnp.maximum(me_m - 1, 0) * count + me_t), 8)
    above = got[pl.ds(at, 16), :] * (me_m > 0).astype(F32)
    at = pl.multiple_of(FIRST * (jnp.minimum(me_m + 1, n_mel - 1) * count + me_t), 8)
    below = got[pl.ds(at, 16), :] * (me_m < n_mel - 1).astype(F32)
    above = jnp.concatenate([above[4:8], above[12:16]], axis=1)
    below = jnp.concatenate([below[0:4], below[8:12]], axis=1)
    own = spec[0].astype(F32) * usable[:, :frame_dev]
    at = pl.multiple_of(8 * jnp.minimum(me_t + 1, count - 1), 8)
    after = strips[pl.ds(at, 8), :][:, :mels] * (me_t + 1 < count).astype(F32)
    at = pl.multiple_of(8 * jnp.maximum(me_t - 1, 0), 8)
    before = strips[pl.ds(at, 8), :][:, :mels] * (me_t > 0).astype(F32)
    sides = jnp.concatenate([after[0:4], before[4:8], jnp.zeros((8, mels), F32)], axis=0).astype(BF16)
    side = iota((16, RIM), 0)
    place = iota((16, RIM), 1) == jnp.where(side < 4, side, jnp.where(side < 8, side + RIM - 8, -1))
    halo[0:8] = jnp.zeros((8, RIM), F32)
    halo[mels : mels + 8] = jnp.zeros((8, RIM), F32)
    halo[4 : mels + 4] = dot(sides, place.astype(BF16), ((0,), (0,)))
    rim = halo[pl.ds(pl.multiple_of(me_m * rows, 8), BAND), :]
    near = jnp.concatenate([jnp.concatenate([above, own, below], axis=0), rim], axis=1)
    x3[...] = jnp.concatenate(
        [
            pltpu.roll(near, 1, 1) * behind,
            near,
            pltpu.roll(near, wide - 1, 1) * ahead,
            jnp.broadcast_to(usable, (BAND, wide)),
            jnp.zeros((128 - 4 * BAND, wide), F32),
        ],
        axis=0,
    ).astype(BF16)
    pre_one[...] = dot(w1[...], x3[...])
    lane = iota((1, 128), 1)
    parts = jnp.where(lane < 92, every(SUMS) + every(SUMS + 1) + every(SUMS + 2), 0.0)
    centres, numbers = parts[:, 90:91], parts[:, 91:92]
    centre = jnp.sum(centres * numbers, axis=0, keepdims=True)
    centre = centre / jnp.maximum(jnp.sum(numbers, axis=0, keepdims=True), 1.0)
    delta = centres - centre
    features = jnp.sum(parts + delta * numbers * jnp.where(lane < 81, delta, 1.0), axis=0, keepdims=True)
    moved = jnp.sum(delta * parts, axis=0, keepdims=True)
    def edge_row(k, n):
        first = FIRST * k * count + n
        return jnp.concatenate(
            [got[pl.ds(first, count, stride=FIRST), :], got[pl.ds(first + 8, count, stride=FIRST), :]], axis=1
        )

    edge_rows = [[edge_row(k, n) for n in (0, 1, 6, 7)] for k in range(n_mel)]
    zero = jnp.zeros((count, frame_dev), F32)
    rows_of = [[], [], []]
    for k, (top, second, fore, bottom) in enumerate(edge_rows):
        for n, v in enumerate((edge_rows[k - 1][3] if k else zero, top, second)):
            rows_of[n].append(v)
        for n, v in enumerate((fore, bottom, edge_rows[k + 1][0] if k + 1 < n_mel else zero)):
            rows_of[n].append(v)
    f_usable, f_behind, f_ahead = (all_masks[n * count : (n + 1) * count, :] for n in range(3))
    lane = iota((count, frame_dev), 1)

    def frame_before(v):
        v = pltpu.roll(v, 1, 1)
        return jnp.where(lane == 0, pltpu.roll(v, 1, 0), v) * f_behind

    def frame_after(v):
        v = pltpu.roll(v, frame_dev - 1, 1)
        return jnp.where(lane == frame_dev - 1, pltpu.roll(v, count - 1, 0), v) * f_ahead

    taps = []
    for group in rows_of:
        for move in (frame_before, lambda v: v, frame_after):
            taps.append(jnp.concatenate([move(v) for v in group], axis=1))
    f_usable = jnp.concatenate([f_usable] * (2 * n_mel), axis=1)
    borders = (taps, f_usable)
    edge = strips[...]
    q_usable, q_behind, q_ahead = (edge_masks[:, n : n + 1] for n in range(3))
    lane = iota((count * 8, 128), 1)
    inside = (lane < mels) & (lane % rows != 0) & (lane % rows != rows - 1)
    shifted = [
        pltpu.roll(edge, 1, 0) * q_behind,
        edge,
        pltpu.roll(edge, count * 8 - 1, 0) * q_ahead,
    ]
    taps = [pltpu.roll(v, (1 - i) % 128, 1) if i != 1 else v for i in range(3) for v in shifted]
    features = features + feature_rows(centre, borders, (taps, jnp.where(inside, q_usable, 0.0)))
    features = jnp.where(iota((1, 128), 1) < 90, features, 0.0)
    near_mean = jnp.sum(singles[...] * features, axis=1, keepdims=True) / total
    around = jnp.sum(singles[...], axis=1, keepdims=True)
    square = jnp.sum(pairs[...] * features, axis=1, keepdims=True)
    square = (square + 2.0 * around * jnp.sum(singles[...] * moved, axis=1, keepdims=True)) / total
    inv = lax.rsqrt(square - near_mean * near_mean + 1e-05)
    mean = near_mean + centre * around
    lane = iota((chan, 128), 1)
    stats[0:chan] = jnp.where(lane == 0, mean, jnp.where(lane == 1, inv, 0.0))
    stats[chan : chan + 8] = jnp.broadcast_to(to_lanes(near_mean), (8, 128))
    stats[chan + 8 : chan + 16] = jnp.broadcast_to(to_lanes(inv), (8, 128))
    scale = 0.5 * to_column(params[0:1], chan) * inv
    shift = 0.5 * to_column(params[1:2], chan) - mean * scale
    stats[chan + 16 :] = jnp.where(lane == 0, scale, jnp.where(lane == 1, shift, 0.0))
    scale = jnp.broadcast_to(scale, (chan, wide))
    shift = jnp.broadcast_to(shift, (chan, wide))
    ext = w1.shape[0] // chan
    block, taps = wf.shape
    first = jnp.zeros((chan, 128), F32)
    second = jnp.zeros((chan, 128), F32)
    own_mask = usable[:, :frame_dev]
    low_masks = [m.astype(BF16) for m in (usable, behind, ahead)]
    for r in range(ext):
        value, _ = silu_halves(pre_one[r * chan : (r + 1) * chan, :] * scale + shift)
        if not 0 <= r - 3 < rows:
            value = value * row_valid(r - 3, rows)
        base = r * 3 * chan
        low = value.astype(BF16) * low_masks[0]
        act[base : base + chan, :], act[base + 2 * chan : base + 3 * chan, :] = shifted_frames(low, *low_masks[1:])
        act[base + chan : base + 2 * chan, :] = low
        if r < 3 or r % 2 == 0:
            continue
        g = (r - 3) // 2
        result = dot(wf[...], act[g * 3 * block : g * 3 * block + taps, :frame_dev])
        pre_two[g * block : (g + 1) * block, :frame_dev] = result
        if g % 2:
            beside = [act[n * 3 * block : n * 3 * block + taps, frame_dev:] for n in (g - 1, g)]
            beside = dot(wf[...], jnp.concatenate(beside, axis=1))
            for n in range(2):
                pre_two[(g - 1 + n) * block : (g + n) * block, frame_dev:] = beside[:, n * RIM : (n + 1) * RIM]
        for q in range(2):
            if 2 <= 2 * g + q < rows + 2:
                p = result[q * chan : (q + 1) * chan]
                masked = p * own_mask
                first = first + halves(masked)
                second = second + halves(masked * p)
    moved = dot(jnp.broadcast_to(moved, (8, 128)), twice[...], precision=EXACT)[0:1]
    features_out[...] = jnp.concatenate(
        [features + moved, jnp.broadcast_to(centre, (1, 128)), jnp.zeros((6, 128), F32)], axis=0
    )
    share = share_of(devices, chan)

    def put(n, value):
        rows_out[pl.ds(n, devices, stride=SECOND), :] = jnp.broadcast_to(value, (devices, 128))

    for n in range(share):
        put(3 + n, moved_rows(every(EDGES + share + n), count))
        put(3 + share + n, moved_rows(every(EDGES + n), -count))
    for n in [0, 1, 2] + list(range(3 + 2 * share, SECOND - 1)):
        put(n, jnp.zeros((1, 128), F32))
    lane = iota((devices, 128), 1)
    tm = iota((devices, 128), 0) % count
    lefts = jnp.where(lane >= SIDE, every(SUMS), 0.0)
    rights = jnp.where(lane >= SIDE, every(SUMS + 1), 0.0)
    beside = jnp.zeros((devices, 128), F32)
    for n, step in enumerate((0, count, -count)):
        one = jnp.where(tm > 0, moved_rows(rights, step + 1), 0.0)
        two = jnp.where(tm < count - 1, moved_rows(lefts, step - 1), 0.0)
        beside = beside + pltpu.roll(one, (32 * n - SIDE) % 128, 1) + pltpu.roll(two, (32 * n + 16 - SIDE) % 128, 1)
    put(SECOND - 1, beside)
    first = jnp.sum(first, axis=1, keepdims=True)
    second = jnp.sum(second, axis=1, keepdims=True)
    parts = list(three_parts(to_lanes(first) + to_lanes(second, chan)))
    parts = jnp.concatenate(parts + [jnp.zeros((SECOND - 3, 128), F32)], axis=0)
    for d in range(devices):
        payload[d] = (rows_out[SECOND * d : SECOND * (d + 1), :] + parts).astype(BF16)


def spreading(half):
    lane = iota((half, 2 * half), 1)
    return jnp.where(lane >> 1 == iota((half, 2 * half), 0), 0.25, 0.0).astype(BF16)


def half_share(devices, taps):
    return -(-taps // 2 // devices)


def backward_scaled(recv, pre_two, act, own_rows, params, masks,
                    grad, kept_half, sent_half, totals, stats, up, right, got, halved):
    devices = recv.shape[0]
    got[...] = recv[:, 0:SECOND, :].astype(F32).reshape(devices * SECOND, 128)
    chan = params.shape[1]
    half = own_rows.shape[1]
    frame_dev = 2 * half
    rows = MEL_ROWS
    up[...] = dot(own_rows[...], spreading(half))
    usable = masks[0:1, :frame_dev]
    total = masks[3:4, 0:1]
    sums = [got[pl.ds(n, devices, stride=SECOND), :] for n in range(3)]
    sums = jnp.sum(sums[0] + sums[1] + sums[2], axis=0, keepdims=True)
    mean = to_column(sums, chan) / total
    inv = lax.rsqrt(to_column(sums, chan, chan) / total - mean * mean + 1e-05)
    scale = 0.5 * to_column(params[2:3], chan) * inv
    shift = 0.5 * to_column(params[3:4], chan) - mean * scale
    lane = iota((chan, 128), 1)
    columns = jnp.zeros((chan, 128), F32)
    for n, column in enumerate((mean, inv, scale, shift)):
        columns = jnp.where(lane == n, column, columns)
    stats[0:chan] = columns
    stats[chan : chan + 8] = jnp.broadcast_to(to_lanes(inv), (8, 128))
    mean, inv, scale, shift = (jnp.broadcast_to(v, (chan, frame_dev)) for v in (mean, inv, scale, shift))
    first = jnp.zeros((chan, 128), F32)
    second = jnp.zeros((chan, 128), F32)
    mask = 0.5 * usable
    right[3 * chan :] = jnp.ones((16, rows * frame_dev), BF16)
    table = jnp.zeros((9 * chan, 3 * chan + 16), F32)
    for m in range(rows):
        at = slice(m * chan, (m + 1) * chan)
        pre = pre_two[(m + 2) * chan : (m + 3) * chan, :frame_dev]
        _, slope = silu_halves(pre * scale + shift)
        g = up[m // 2 * chan : (m // 2 + 1) * chan, :] * slope * mask
        grad[at, :] = g
        normed = (pre - mean) * inv
        first = first + halves(g * normed)
        second = second + halves(g)
        lanes = slice(m * frame_dev, (m + 1) * frame_dev)
        right[0:chan, lanes] = g.astype(BF16)
        right[chan : 2 * chan, lanes] = normed.astype(BF16)
        right[2 * chan : 3 * chan, lanes] = (g - right[0:chan, lanes].astype(F32)).astype(BF16)
        if m in (5, 11, rows - 1):
            start = m - m % 6
            left = [act[(n + 2) * 3 * chan : (n + 5) * 3 * chan, :frame_dev] for n in range(start, m + 1)]
            lanes = slice(start * frame_dev, (m + 1) * frame_dev)
            table = table + dot(jnp.concatenate(left, axis=1), right[:, lanes], ((1,), (1,)))
    first = jnp.sum(first, axis=1, keepdims=True)
    second = jnp.sum(second, axis=1, keepdims=True)
    totals[...] = jnp.broadcast_to(to_lanes(first) + to_lanes(second, chan), (8, 128))
    rest = jnp.concatenate([table[:, 2 * chan :], jnp.zeros((9 * chan, chan - 16), F32)], axis=1)
    both = table[:, : 2 * chan] + jnp.where(iota(rest.shape, 1) < chan, rest, 0.0)
    single = rest[:, chan : chan + 1]
    taps = 9 * chan // 2
    lane = iota((devices, 128), 1)
    for h in range(2):
        halved[h, 0:taps] = both[h * taps : (h + 1) * taps]
        constants = jnp.zeros((devices, 128), F32)
        for k in range(half_share(devices, 9 * chan)):
            at = h * taps + k * devices
            ones = single[at : min(at + devices, (h + 1) * taps)]
            if ones.shape[0] < devices:
                ones = jnp.concatenate([ones, jnp.zeros((devices - ones.shape[0], 1), F32)], axis=0)
            constants = jnp.where(lane == k, ones, constants)
        halved[h, taps:] = constants
    core = lax.axis_index("tm") % 2
    kept_half[...] = halved[core]
    sent_half[...] = halved[1 - core]


def around(recv, pre_two, masks, stats, ring, rim, pairs, sides, up, got, beyond):
    devices = recv.shape[0]
    got[...] = recv[:, 0:SECOND, :].astype(F32).reshape(devices * SECOND, 128)
    rows = MEL_ROWS
    many = rows // 2
    wide = pre_two.shape[1]
    frame_dev = wide - RIM
    chan = pre_two.shape[0] // (rows + 4)
    usable = masks[0:1]
    share = share_of(devices, chan)
    holders = chan // share

    def every(n):
        return got[pl.ds(n, devices, stride=SECOND), :]

    beside = every(SECOND - 1)[:holders]
    lane = iota((holders, RIM), 1)
    for n in range(share):
        first = n * holders
        beyond[first : first + holders, :] = every(3 + n)[:holders]
        beyond[chan + first : chan + first + holders, :] = every(3 + share + n)[:holders]
        for r in range(many + 2):
            at = many * n + (r if r < many else 32 + many - 1 if r == many else 64)
            left, right_of = beside[:, at : at + 1], beside[:, at + 16 : at + 17]
            side = jnp.where(lane >= RIM - 2, 0.25 * left, jnp.where(lane < 2, 0.25 * right_of, 0.0))
            sides[r * chan + first : r * chan + first + holders, :] = side
    up[...] = dot(beyond[...].astype(BF16), spreading(frame_dev // 2))
    scale = jnp.broadcast_to(stats[0:chan, 2:3], (chan, wide))
    shift = jnp.broadcast_to(stats[0:chan, 3:4], (chan, wide))
    for n, m in enumerate((-2, -1, rows, rows + 1)):
        below = n // 2
        upstream = jnp.concatenate(
            [
                up[below * chan : (below + 1) * chan, :],
                sides[(many + below) * chan : (many + below + 1) * chan, :],
            ],
            axis=1,
        )
        _, slope = silu_halves(pre_two[(m + 2) * chan : (m + 3) * chan, :] * scale + shift)
        ring[n * chan : (n + 1) * chan, :] = upstream * slope * (usable * (0.5 * row_valid(m, rows)))
    both = None
    for m in range(rows):
        at = slice((m + 2) * chan, (m + 3) * chan)
        _, slope = silu_halves(pre_two[at, frame_dev:] * scale[:, frame_dev:] + shift[:, frame_dev:])
        upstream = sides[m // 2 * chan : (m // 2 + 1) * chan, :]
        rim[m * chan : (m + 1) * chan, :] = upstream * slope * (0.5 * usable[:, frame_dev:])
        value, _ = silu_halves(pre_two[at, :frame_dev] * scale[:, :frame_dev] + shift[:, :frame_dev])
        value = value * usable[:, :frame_dev]
        both = value if m % 2 == 0 else both + value
        if m % 2:
            pairs[m // 2 * chan : (m // 2 + 1) * chan, :] = both


def pack_sums(kept_half, received, totals, after, payload):
    del after
    devices = kept_half.shape[0] - TAPS // 2
    block = payload.shape[0] // devices
    payload[pl.ds(0, devices, stride=block), :] = jnp.broadcast_to(totals[0:1], (devices, 128))
    taps = TAPS // 2
    total = kept_half[...] + received[...]
    for k in range(block - 2):
        cut = total[k * devices : min((k + 1) * devices, taps)]
        if cut.shape[0] < devices:
            cut = jnp.concatenate([cut, jnp.zeros((devices - cut.shape[0], 128), F32)], axis=0)
        payload[pl.ds(1 + k, devices, stride=block), :] = cut
    payload[pl.ds(block - 1, devices, stride=block), :] = total[taps:]


def pool(totals, pairs, out, gain_out, bias_out, temp):
    gain_out[...] = totals[0:1, : gain_out.shape[1]]
    bias_out[...] = totals[0:1, gain_out.shape[1] :]
    chan, rows, half = out.shape[1:]
    to_mean = jnp.where(iota((2 * half, half), 0) >> 1 == iota((2 * half, half), 1), 0.25, 0.0)
    pooled = dot(pairs[...], to_mean, precision=EXACT)
    for r in range(rows):
        temp[pl.ds(r, chan, stride=rows), :] = pooled[r * chan : (r + 1) * chan]
    out[0] = temp[...].reshape(chan, rows, half).astype(BF16)


def backward(recv, pre_two, grad, ring, rim, stats_two, w1, x3, stats, params, masks, wb,
             out, own_low, payload, totals, g3, pre_one, g1):
    chan = params.shape[1]
    rows = MEL_ROWS
    wide = pre_two.shape[1]
    frame_dev = wide - RIM
    usable = masks[0:1]
    behind, ahead = (masks[n : n + 1].astype(BF16) for n in (1, 2))
    total = masks[3:4, 0:1]
    devices = payload.shape[0] // 14
    pre_one[...] = dot(w1[3 * chan : (rows + 3) * chan], x3[:, :frame_dev])

    even, odd = summed_blocks(recv, devices, 2)
    sums = even[0:1] + odd[0:1]
    gain_sum, bias_sum = sums[:, :chan], sums[:, chan:]
    totals[...] = jnp.broadcast_to(sums, (8, 128))
    mean, inv = stats_two[0:chan, 0:1], stats_two[0:chan, 1:2]
    factor = to_column(params[2:3], chan) * inv
    gain_part = factor * (to_column(sums, chan) / total * inv)
    bias_part = factor * (to_column(sums, chan, chan) / total) - mean * gain_part
    gain_part = jnp.broadcast_to(gain_part, (chan, wide))
    bias_part = jnp.broadcast_to(bias_part, (chan, wide))
    factor = jnp.broadcast_to(factor, (chan, wide))
    scale = jnp.broadcast_to(stats[chan + 16 :, 0:1], (chan, frame_dev))
    shift = jnp.broadcast_to(stats[chan + 16 :, 1:2], (chan, frame_dev))
    factor_one = jnp.broadcast_to(to_column(params[0:1], chan) * stats[0:chan, 1:2], (chan, frame_dev))
    own_mask = 0.5 * usable[:, :frame_dev]
    count = pre_two.shape[0] // chan
    table = jnp.zeros((chan, 128), F32)

    def tap_sums(m):
        part = g1[m * chan : (m + 4) * chan, :]
        high = lax.reduce_precision(part, 8, 7)
        low = (part - high).astype(BF16)
        taps_in = x3[:, :frame_dev]
        products = dot(high.astype(BF16), taps_in, ((1,), (1,))) + dot(low, taps_in, ((1,), (1,)))
        moved = [pltpu.roll(products[k * chan : (k + 1) * chan], 128 - (m + k + 3), 1) for k in range(4)]
        return (moved[0] + moved[1]) + (moved[2] + moved[3])

    for q in range(count):
        at = slice(q * chan, (q + 1) * chan)
        mask = usable if 0 <= q - 2 < rows else usable * row_valid(q - 2, rows)
        if 2 <= q < rows + 2:
            own = slice((q - 2) * chan, (q - 1) * chan)
            scaled = jnp.concatenate([grad[own, :], rim[own, :]], axis=1)
        else:
            n = q if q < 2 else q - rows
            scaled = ring[n * chan : (n + 1) * chan, :]
        low = (factor * scaled - (bias_part + pre_two[at, :] * gain_part) * mask).astype(BF16)
        out[at, :] = low
        if not 1 <= q < count - 1:
            continue
        base = (q - 1) * 3 * chan
        for n, v in enumerate((low,) + shifted_frames(low, behind, ahead)):
            spot = base + (1, 0, 2)[n] * chan
            g3[spot : spot + chan, :] = v[:, :frame_dev]
        start = q - 4
        if start < 0 or start % 2:
            continue
        result = dot(wb[...], g3[start * 3 * chan : (start + 4) * 3 * chan, :])
        for n in range(2):
            m = start + n
            at = slice(m * chan, (m + 1) * chan)
            _, slope = silu_halves(pre_one[at, :] * scale + shift)
            value = result[n * chan : (n + 1) * chan] * slope * own_mask
            own_low[at, :] = (value * factor_one).astype(BF16)
            g1[at, :] = value
        if start % 4 == 2 and start > 2:
            table = table + tap_sums(start - 6)
    table = table + tap_sums(rows - 4)
    table = table.T
    places = [BAND * j + i for i in range(3) for j in range(3)] + [3 * BAND]
    rows10 = jnp.concatenate([table[n : n + 1] for n in places], axis=0)
    share = even.shape[0] - 2
    mine = jnp.concatenate([even[1 : share + 1], odd[1 : share + 1]], axis=0)
    single = jnp.concatenate([to_column(v[share + 1 :], share) for v in (even, odd)], axis=0)
    factor_l = params[2:3] * stats_two[chan : chan + 1, :chan]
    mine = mine[:, :chan] - (bias_sum * single + gain_sum * mine[:, chan:]) / total
    mine = factor_l * mine
    mine = jnp.concatenate([mine[:share], mine[share:]], axis=1)
    if share < 9:
        mine = jnp.concatenate([mine, jnp.zeros((9 - share, 128), F32)], axis=0)
    sums = jnp.concatenate([rows10[0:5], rows10[5:10]], axis=1)
    block = jnp.concatenate([sums, mine], axis=0)
    block = jnp.concatenate([block] * 4, axis=0)
    for d in range(0, devices, 4):
        payload[14 * d : 14 * (d + 4), :] = block


def transposed(grad, own_low, w1, wb, x3, stats, features, k1t, params, masks, ws_hbm,
               first, ws, normed_taps, low, g3, rim, sem):
    load = pltpu.make_async_copy(ws_hbm, ws, sem)
    load.start()
    rows = MEL_ROWS
    chan = own_low.shape[0] // rows
    wide = grad.shape[1]
    frame_dev = wide - RIM
    count = grad.shape[0] // chan
    usable = masks[0:1]
    behind, ahead = (masks[n : n + 1].astype(BF16) for n in (1, 2))
    scale = jnp.broadcast_to(stats[chan + 16 :, 0:1], (chan, wide))
    shift = jnp.broadcast_to(stats[chan + 16 :, 1:2], (chan, wide))
    factor = jnp.broadcast_to(to_column(params[0:1], chan) * stats[0:chan, 1:2], (chan, wide))
    edge = (0, 1, 2, 3, count - 4, count - 3, count - 2, count - 1)
    for q in range(count):
        value = grad[q * chan : (q + 1) * chan, :]
        for n, v in enumerate((value,) + shifted_frames(value, behind, ahead)):
            spot = (3 * q + (1, 0, 2)[n]) * chan
            rim[spot : spot + chan, :] = v[:, frame_dev:]
            if q in edge:
                spot = (3 * edge.index(q) + (1, 0, 2)[n]) * chan
                g3[spot : spot + chan, :] = v[:, :frame_dev]
    low[chan : (rows + 1) * chan, :frame_dev] = own_low[...]

    def put(m, lanes, result, pre_one):
        at = slice((m + 1) * chan, (m + 2) * chan)
        _, slope = silu_halves(pre_one * scale[:, lanes] + shift[:, lanes])
        mask = usable[:, lanes] * (0.5 * row_valid(m, rows))
        low[at, lanes] = (result * slope * mask * factor[:, lanes]).astype(BF16)

    pre_one = dot(w1[2 * chan : (rows + 4) * chan, :], x3[:, frame_dev:])
    beside = slice(frame_dev, wide)
    for start in range(0, rows + 2, 2):
        result = dot(wb[...], rim[start * 3 * chan : (start + 4) * 3 * chan, :])
        for n in range(2):
            at = slice((start + n) * chan, (start + n + 1) * chan)
            put(start + n - 1, beside, result[n * chan : (n + 1) * chan], pre_one[at])
    own = slice(0, frame_dev)
    result = dot(wb[...], g3[: 4 * 3 * chan, :])
    put(-1, own, result[:chan], dot(w1[2 * chan : 3 * chan, :], x3[:, :frame_dev]))
    result = dot(wb[...], g3[4 * 3 * chan :, :])
    put(rows, own, result[chan:], dot(w1[(rows + 3) * chan : (rows + 4) * chan, :], x3[:, :frame_dev]))
    row = features[0:1, :]
    lane = iota((1, 128), 1)
    gram = jnp.concatenate(
        [jnp.where(lane < 9, pltpu.roll(row, 128 - 9 * t, 1) if t else row, 0.0) for t in range(9)]
        + [jnp.zeros((7, 128), F32)],
        axis=0,
    )
    single = to_column(row, 16, 81)[0:9]
    k_rows = jnp.concatenate([k1t[...], jnp.zeros((112, chan), F32)], axis=0)
    mean_l, inv_l = stats[chan : chan + 1, :chan], stats[chan + 8 : chan + 9, :chan]
    normed = inv_l * (dot(gram, k_rows, precision=EXACT)[0:9] - single * mean_l)
    normed_taps[0:16] = jnp.concatenate([normed, jnp.zeros((7, chan), F32)], axis=0)
    normed_taps[16:32] = jnp.broadcast_to(to_column(row, 16, 81), (16, chan))
    load.wait()
    first[...] = dot(ws[...], low[...])


def finish(recv, features, stats, k1t, first, ws, w1, x3, normed_taps, params, masks,
           spec_hbm, kernel_one_hbm, kernel_two_hbm, gain_hbm, bias_hbm,
           spec_grad, kernel_one, kernel_two, gain_out, bias_out, sems):
    chan = params.shape[1]
    rows = MEL_ROWS
    wide = x3.shape[1]
    frame_dev = wide - RIM
    usable, behind, ahead = (masks[n : n + 1] for n in range(3))
    total = masks[3:4, 0:1]
    gain = params[0:1]
    count = recv.shape[0] // 14
    share = half_share(count, 9 * chan)
    left = [recv[pl.ds(5 + p, count, stride=14), :] for p in range(share)]
    taps = TAPS // 2
    whole = [jnp.concatenate([v[:, h * chan : (h + 1) * chan] for v in left], axis=0)[:taps] for h in range(2)]
    whole = jnp.concatenate(whole, axis=0)
    for t in range(9):
        kernel_two[t] = whole[t * chan : (t + 1) * chan].T
    stores = [pltpu.make_async_copy(kernel_two, kernel_two_hbm, sems.at[4])]
    stores[0].start()
    sums = summed_blocks(recv, count)[0:5]
    ten = jnp.concatenate([sums[:, :chan], sums[:, chan:]], axis=0)
    bias_sum = ten[9:10]
    mean_l, inv_l = stats[chan : chan + 1, :chan], stats[chan + 8 : chan + 9, :chan]
    ten = ten - features[1:2, 0:1] * bias_sum
    k = k1t[0:9]
    gain_sum = inv_l * (jnp.sum(k * ten[0:9], axis=0, keepdims=True) - mean_l * bias_sum)
    gain_out[...] = gain_sum
    bias_out[...] = bias_sum
    factor_l = gain * inv_l
    scale = factor_l * gain_sum / total * inv_l
    scale = jnp.concatenate(
        [scale * row_valid(-1, rows)] + [scale] * rows + [scale * row_valid(rows, rows)], axis=1
    )
    many = 3 * rows

    def in_parts(v, right):
        high = lax.reduce_precision(v, 8, 7)
        v = dot(jnp.concatenate([high, v - high], axis=0).astype(BF16), right)
        return v[:many] + v[many:]

    taken = in_parts(in_parts(ws[...].astype(F32) * scale, w1[2 * chan : (rows + 4) * chan, :]), x3[...])
    taps = first[...] - taken
    moved = [taps[rows * b : rows * (b + 1)] for b in range(3)]
    mean_full = mean_l + features[1:2, 0:1] * jnp.sum(k, axis=0, keepdims=True)
    constant = jnp.sum(k * (factor_l * (bias_sum - gain_sum * inv_l * mean_full) / total), axis=1, keepdims=True)
    for a in range(3):
        row = iota((rows, 1), 0) + (a - 1) + lax.axis_index("mel") * rows
        valid = ((row >= 0) & (row < lax.axis_size("mel") * rows)).astype(F32) * usable
        for b in range(3):
            t = 3 * (2 - a) + 2 - b
            moved[b] = moved[b] - constant[t : t + 1] * valid
    result = pltpu.roll(moved[0], 1, 1) * behind + moved[1] + pltpu.roll(moved[2], wide - 1, 1) * ahead
    spec_grad[0] = (result * usable)[:, :frame_dev]
    grad_taps = factor_l * (ten[0:9] - (bias_sum * normed_taps[16:25] + gain_sum * normed_taps[0:9]) / total)
    for i in range(3):
        kernel_one[i] = grad_taps[3 * i : 3 * i + 3]
    outs = ((spec_grad, spec_hbm), (kernel_one, kernel_one_hbm), (gain_out, gain_hbm), (bias_out, bias_hbm))
    wait_all(stores + start_all(*outs, sems=sems))


def run(kernel, outs, scratch, *args, hbm=0, apart=(), flops=10**8, size=4 * 10**6):
    vmem = pl.BlockSpec(memory_space=pltpu.VMEM)
    devices = lax.axis_size("mel") * lax.axis_size("tm")
    specs = []
    args = list(args)
    for n, a in enumerate(args):
        if hbm and n >= len(args) - hbm:
            specs.append(pl.BlockSpec(memory_space=pltpu.HBM))
            args[n] = pltpu.with_memory_space_constraint(a, pltpu.HBM)
        else:
            specs.append(vmem)
            args[n] = pltpu.with_memory_space_constraint(a, pltpu.VMEM)
    return pl.pallas_call(
        kernel,
        out_shape=outs,
        in_specs=specs,
        out_specs=[pl.BlockSpec(memory_space=pltpu.HBM) if n in apart else vmem for n in range(len(outs))],
        scratch_shapes=scratch,
        compiler_params=pltpu.CompilerParams(vmem_limit_bytes=(29 + devices // 32) * 2**20),
        cost_estimate=pl.CostEstimate(flops=flops, bytes_accessed=size, transcendentals=0),
    )(*args)


def shape(dims, dtype=F32):
    return jax.ShapeDtypeStruct(dims, dtype)


def kept(dims, dtype=F32):
    return pltpu.VMEM(dims, dtype)


def far(dims, dtype=F32):
    return pltpu.HBM(dims, dtype)


def exchange(blocks, axes=AXES):
    return lax.all_to_all(blocks, axes, 0, 0, tiled=True)


def exchange_rows(rows, axes=AXES):
    return exchange(rows[:, None, :], axes)[:, 0, :]


def shards(spectrum, clip_bounds, kernel_one, gain_one, bias_one, kernel_two, gain_two, bias_two, pooled_grad):
    _, rows, frame_dev = spectrum.shape
    chan = kernel_two.shape[0]
    n_mel, n_tm = lax.axis_size("mel"), lax.axis_size("tm")
    devices = n_mel * n_tm
    half = frame_dev // 2
    wide = frame_dev + RIM
    mels = n_mel * rows

    packed, own, spec, masks = run(
        pack,
        [
            kept((devices, FIRST, 128), BF16),
            kept(pooled_grad.shape, BF16),
            kept(spectrum.shape, BF16),
            kept((8, wide)),
        ],
        [
            pltpu.SMEM(clip_bounds.shape, jnp.int32),
            pltpu.VMEM((2 * chan, half), F32),
            pltpu.VMEM((devices * FIRST, 128), F32),
            pltpu.SemaphoreType.DMA((3,)),
        ],
        spectrum,
        pooled_grad,
        clip_bounds,
        hbm=3,
    )
    recv = exchange(packed)
    ext = rows + 6
    span = 4 * 3 * chan
    wf, wb, w1, ws, pairs, singles, k1t, params, all_masks, edge_masks, twice, own_rows = run(
        weights,
        [
            kept((2 * chan, span), BF16),
            kept((2 * chan, span), BF16),
            kept((ext * chan, 128), BF16),
            far((rows * 3, (rows + 2) * chan), BF16),
            kept((chan, 128)),
            kept((chan, 128)),
            kept((16, chan)),
            kept((8, chan)),
            kept((3 * n_tm, frame_dev)),
            kept((n_tm * 8, 128)),
            kept((128, 128)),
            kept((chan * rows // 2, half), BF16),
        ],
        [
            pltpu.VMEM((9, chan, chan), BF16),
            pltpu.VMEM((3, 3, chan), BF16),
            pltpu.VMEM((4, 1, chan), F32),
            pltpu.SMEM(clip_bounds.shape, jnp.int32),
            pltpu.VMEM((rows * 3, (rows + 2) * chan), BF16),
            pltpu.VMEM((chan * rows // 2, half), F32),
            pltpu.SemaphoreType.DMA((8,)),
        ],
        own,
        clip_bounds,
        jnp.transpose(kernel_two, (2, 3, 0, 1)).reshape(9, chan, chan),
        jnp.transpose(kernel_one, (1, 2, 0)),
        gain_one[None],
        bias_one[None],
        gain_two[None],
        bias_two[None],
        hbm=7,
        apart=(3,),
    )
    pre_two, payload, act, x3, stats_one, features = run(
        forward_one,
        [
            kept(((rows + 4) * chan, wide)),
            kept((devices, SECOND, 128), BF16),
            kept((ext * 3 * chan, wide), BF16),
            kept((128, wide), BF16),
            kept((2 * chan + 16, 128)),
            kept((8, 128)),
        ],
        [
            pltpu.VMEM((ext * chan, wide), F32),
            pltpu.VMEM((devices * FIRST, 128), F32),
            pltpu.VMEM((n_tm * 8, 128), F32),
            pltpu.VMEM((mels + 8, RIM), F32),
            pltpu.VMEM((devices * SECOND, 128), F32),
        ],
        recv,
        spec,
        pairs,
        singles,
        twice,
        w1,
        wf,
        params,
        masks,
        all_masks,
        edge_masks,
    )
    recv = exchange(payload)
    grad, kept_half, sent_half, totals, stats_two = run(
        backward_scaled,
        [
            kept((rows * chan, frame_dev)),
            kept((TAPS // 2 + devices, 128)),
            kept((TAPS // 2 + devices, 128)),
            kept((8, 128)),
            kept((chan + 8, 128)),
        ],
        [
            pltpu.VMEM((rows // 2 * chan, frame_dev), F32),
            pltpu.VMEM((3 * chan + 16, rows * frame_dev), BF16),
            pltpu.VMEM((devices * SECOND, 128), F32),
            pltpu.VMEM((2, TAPS // 2 + devices, 128), F32),
        ],
        recv,
        pre_two,
        act,
        own_rows,
        params,
        masks,
    )
    received = lax.ppermute(sent_half, "tm", [(i, i ^ 1) for i in range(n_tm)])
    ring, rim, row_pairs = run(
        around,
        [kept((4 * chan, wide)), kept((rows * chan, RIM)), kept((rows // 2 * chan, frame_dev))],
        [
            pltpu.VMEM(((rows // 2 + 2) * chan, RIM), F32),
            pltpu.VMEM((2 * chan, frame_dev), F32),
            pltpu.VMEM((devices * SECOND, 128), F32),
            pltpu.VMEM((2 * chan, half), F32),
        ],
        recv,
        pre_two,
        masks,
        stats_two,
    )
    (payload,) = run(
        pack_sums,
        [kept((devices * (half_share(devices, 9 * chan) + 2), 128))],
        [],
        kept_half,
        received,
        totals,
        rim,
    )
    recv = exchange_rows(payload)
    grad, own_low, payload, totals = run(
        backward,
        [
            kept(((rows + 4) * chan, wide), BF16),
            kept((rows * chan, frame_dev), BF16),
            kept((devices * 14, 128)),
            kept((8, 128)),
        ],
        [
            pltpu.VMEM(((rows + 2) * 3 * chan, frame_dev), BF16),
            pltpu.VMEM((rows * chan, frame_dev), F32),
            pltpu.VMEM((rows * chan, frame_dev), F32),
        ],
        recv,
        pre_two,
        grad,
        ring,
        rim,
        stats_two,
        w1,
        x3,
        stats_one,
        params,
        masks,
        wb,
    )
    recv = exchange_rows(payload)
    pooled, gain_two_grad, bias_two_grad = run(
        pool,
        [shape((1, chan, rows // 2, half), BF16), shape((1, chan)), shape((1, chan))],
        [
            pltpu.VMEM((rows // 2 * chan, 128), F32),
        ],
        totals,
        row_pairs,
    )
    first, ws, normed_taps = run(
        transposed,
        [
            kept((rows * 3, wide)),
            kept((rows * 3, (rows + 2) * chan), BF16),
            kept((32, chan)),
        ],
        [
            pltpu.VMEM(((rows + 2) * chan, wide), BF16),
            pltpu.VMEM((8 * 3 * chan, frame_dev), BF16),
            pltpu.VMEM(((rows + 4) * 3 * chan, RIM), BF16),
            pltpu.SemaphoreType.DMA,
        ],
        grad,
        own_low,
        w1,
        wb,
        x3,
        stats_one,
        features,
        k1t,
        params,
        masks,
        ws,
        hbm=1,
    )
    spec_grad, kernel_one_grad, kernel_two_grad, gain_one_grad, bias_one_grad = run(
        finish,
        [
            shape((1, rows, frame_dev)),
            shape((3, 3, chan)),
            shape((9, chan, chan)),
            shape((1, chan)),
            shape((1, chan)),
        ],
        [
            pltpu.VMEM((1, rows, frame_dev), F32),
            pltpu.VMEM((3, 3, chan), F32),
            pltpu.VMEM((9, chan, chan), F32),
            pltpu.VMEM((1, chan), F32),
            pltpu.VMEM((1, chan), F32),
            pltpu.SemaphoreType.DMA((5,)),
        ],
        recv,
        features,
        stats_one,
        k1t,
        first,
        ws,
        w1,
        x3,
        normed_taps,
        params,
        masks,
        apart=range(5),
    )
    kernel_two_grad = jnp.transpose(kernel_two_grad.reshape(3, 3, chan, chan), (2, 3, 0, 1))
    return (
        pooled,
        spec_grad,
        jnp.transpose(kernel_one_grad, (2, 0, 1)),
        gain_one_grad[0],
        bias_one_grad[0],
        kernel_two_grad,
        gain_two_grad[0],
        bias_two_grad[0],
    )


def solution(mesh):
    return jax.shard_map(
        shards,
        mesh=mesh,
        in_specs=(
            P(None, "mel", "tm"),
            P(),
            P(),
            P(),
            P(),
            P(),
            P(),
            P(),
            P(None, None, "mel", "tm"),
        ),
        out_specs=(P(None, None, "mel", "tm"), P(None, "mel", "tm"), P(), P(), P(), P(), P(), P()),
        check_vma=False,
    )
```

```python
import math

import jax
import jax.numpy as jnp
from jax import lax
from jax.experimental import pallas as pl
from jax.experimental.pallas import tpu as pltpu
from jax.sharding import PartitionSpec as P

F32 = jnp.float32
BF16 = jnp.bfloat16
AXES = ("mel", "tm")
EXACT = lax.Precision.HIGHEST
RIM = 128
BAND = 24
MEL_ROWS = 16
FIRST = 24
SUMS, EDGES, COLUMNS = 16, 19, 23
SIDE = 96
TAPS = 576
SECOND = 8


def iota(shape, dim):
    return lax.broadcasted_iota(jnp.int32, shape, dim)


def dot(a, b, over=((1,), (0,)), precision=None):
    return lax.dot_general(a, b, (over, ((), ())), precision=precision, preferred_element_type=F32)


def to_column(lanes, count, start=0):
    shape = (count, lanes.shape[1])
    return jnp.sum(jnp.where(iota(shape, 1) == iota(shape, 0) + start, lanes, 0.0), axis=1, keepdims=True)


def to_lanes(column, start=0, width=128):
    shape = (column.shape[0], width)
    return jnp.sum(jnp.where(iota(shape, 1) == iota(shape, 0) + start, column, 0.0), axis=0, keepdims=True)


def halves(v):
    total = v[:, :128]
    for n in range(128, v.shape[1], 128):
        total = total + v[:, n : n + 128]
    return total


def frame_masks(bounds, frames):
    last = bounds.shape[1] - 1

    def living(f):
        return (f >= 0) & (f < bounds[0, last])

    def paired(f):
        both = living(f) & living(f + 1)
        for k in range(1, last):
            both = both & (f + 1 != bounds[0, k])
        return both

    return tuple(m.astype(F32) for m in (living(frames), paired(frames - 1), paired(frames)))


def row_valid(row, rows):
    mel = lax.axis_index("mel") * rows + row
    return ((mel >= 0) & (mel < lax.axis_size("mel") * rows)).astype(F32)


def start_all(*pairs, sems):
    copies = [pltpu.make_async_copy(src, dst, sems.at[n]) for n, (src, dst) in enumerate(pairs)]
    for copy in copies:
        copy.start()
    return copies


def wait_all(copies):
    for copy in copies:
        copy.wait()


def shifted_frames(value, behind, ahead):
    wide = value.shape[1]
    return pltpu.roll(value, 1, 1) * behind, pltpu.roll(value, wide - 1, 1) * ahead


def three_parts(v):
    high = lax.reduce_precision(v, 8, 7)
    mid = lax.reduce_precision(v - high, 8, 7)
    return high, mid, v - high - mid


def share_of(devices, chan):
    return -(-chan // devices)


def pack(spec_hbm, grad_hbm, bounds_hbm, out, own, spec, masks, bounds, edges, rows_out, sems):
    copies = start_all((bounds_hbm, bounds), (spec_hbm, spec), (grad_hbm, own), sems=sems)
    copies[0].wait()
    wide = masks.shape[1]
    frame_dev = wide - RIM
    devices = out.shape[0]
    rows = MEL_ROWS
    lane = iota((1, wide), 1)
    frames = lax.axis_index("tm") * frame_dev + jnp.where(lane < frame_dev + RIM // 2, lane, lane - wide)
    last = bounds.shape[1] - 1
    pixels = (bounds[0, last] * (lax.axis_size("mel") * rows)).astype(F32)
    found = frame_masks(bounds, frames)
    masks[...] = jnp.concatenate(
        list(found) + [jnp.full((1, wide), 1.0) * pixels, jnp.zeros((4, wide), F32)], axis=0
    )
    usable, behind, ahead = (m[:, :frame_dev] for m in found)
    copies[1].wait()
    x = spec[0].astype(F32) * usable
    lane = iota((1, frame_dev), 1)
    row = iota((rows, 1), 0)
    inner = jnp.where((lane > 0) & (lane < frame_dev - 1), usable, 0.0)
    number = (rows - 2) * jnp.sum(inner, axis=1, keepdims=True)
    inner = inner * ((row > 0) & (row < rows - 1)).astype(F32)
    centre = jnp.sum(jnp.sum(x, axis=0, keepdims=True), axis=1, keepdims=True)
    centre = centre / (rows * jnp.maximum(jnp.sum(usable, axis=1, keepdims=True), 1.0))
    centre = lax.reduce_precision(centre, 8, 7)
    shifted = [pltpu.roll(x, 1, 1) * behind, x, pltpu.roll(x, frame_dev - 1, 1) * ahead]
    taps = [pltpu.roll(v, (1 - i) % rows, 0) if i != 1 else v for i in range(3) for v in shifted]
    features = feature_rows(centre, (taps, inner))
    lane = iota((1, 128), 1)
    features = jnp.where(lane == 90, centre, jnp.where(lane == 91, number, features))
    pick = iota((8, frame_dev), 0)
    column = jnp.where(pick < 4, pick, frame_dev - 8 + pick)
    strip = dot((iota((8, frame_dev), 1) == column).astype(BF16), x.astype(BF16), ((1,), (1,)))
    lane = iota((8, 128), 1)
    repeat = (iota((rows, 128), 1) % rows == iota((rows, 128), 0)).astype(BF16)
    strip = jnp.where(lane // rows == iota((8, 128), 0), dot(strip.astype(BF16), repeat), 0.0)
    strip = jnp.sum(strip, axis=0, keepdims=True)

    def put(n, value):
        rows_out[pl.ds(n, devices, stride=FIRST), :] = jnp.broadcast_to(value, (devices, 128))

    near = jnp.concatenate([x[0:4], x[rows - 4 :]], axis=0)
    near = jnp.concatenate([near[:, :128], near[:, 128:]], axis=0)
    for d in range(devices):
        rows_out[FIRST * d : FIRST * d + 16, :] = near
    put(COLUMNS, strip)
    copies[2].wait()
    _, chan, many, half = own.shape
    share = share_of(devices, chan)
    holders = chan // share
    g = own[0].astype(F32)
    edges[0:chan] = g[:, 0, :]
    edges[chan:] = g[:, many - 1, :]

    def spread_out(v):
        if holders < devices:
            v = jnp.concatenate([v, jnp.zeros((devices - holders, 128), F32)], axis=0)
        return v

    for n in range(share):
        put(EDGES + n, spread_out(edges[n * holders : (n + 1) * holders, :]))
        put(EDGES + share + n, spread_out(edges[chan + n * holders : chan + (n + 1) * holders, :]))
    for n in range(2 * share, COLUMNS - EDGES):
        put(EDGES + n, jnp.zeros((1, 128), F32))
    end = iota((8, half), 0)
    at = iota((8, half), 1)
    ends = ((end == 0) & (at == 0)) | ((end == 1) & (at == half - 1))
    columns = dot(ends.astype(BF16), g.reshape(chan * many, half).astype(BF16), ((1,), (1,)))
    group = 128 // many
    source = iota((128, 128), 0)
    lane = iota((group, 128), 1)
    mine = lane // many == iota((group, 128), 0)
    parts = three_parts(features)
    for n in range(2):
        side = jnp.zeros((holders, 128), F32)
        for m in range(share):
            move = (iota((128, 128), 1) == SIDE + many * m + source % many).astype(BF16)
            first = m * holders * many // 128
            block = [columns[n : n + 1, 128 * q : 128 * (q + 1)] for q in range(first, first + holders * many // 128)]
            block = jnp.concatenate([jnp.where(mine, v, 0.0) for v in block], axis=0)
            side = side + dot(block.astype(BF16), move)
        put(SUMS + n, spread_out(side) + parts[n])
    put(SUMS + 2, parts[2])
    out[...] = rows_out[...].reshape(out.shape).astype(BF16)


def weights(own, bounds_hbm, k2_hbm, k1_hbm, gain_one_hbm, bias_one_hbm, gain_two_hbm, bias_two_hbm,
            wf, wb, w1, ws_hbm, pairs, singles, k1t, params, all_masks, edge_masks, twice, own_rows,
            k2, k1, vectors, bounds, ws, temp, sems):
    loads = start_all(
        (bounds_hbm, bounds),
        (k2_hbm, k2),
        (k1_hbm, k1),
        (gain_one_hbm, vectors.at[0]),
        (bias_one_hbm, vectors.at[1]),
        (gain_two_hbm, vectors.at[2]),
        (bias_two_hbm, vectors.at[3]),
        sems=sems,
    )
    _, many, count, half = own.shape
    temp[...] = own[0].astype(F32).reshape(many * count, half)
    for r in range(count):
        own_rows[r * many : (r + 1) * many] = temp[pl.ds(r, many, stride=count), :].astype(BF16)
    wait_all(loads)
    chan = k2.shape[1]
    span = wf.shape[1]
    taps = [k2[t].astype(F32) for t in range(9)]
    rest = jnp.zeros((chan, span - 9 * chan), F32)
    forward = jnp.concatenate(taps + [rest], axis=1)
    backward = jnp.concatenate([taps[8 - t].T for t in range(9)] + [rest], axis=1)
    for r in range(wb.shape[0] // chan):
        at = slice(r * chan, (r + 1) * chan)
        wb[at] = (pltpu.roll(backward, 3 * chan * r, 1) if r else backward).astype(BF16)
    full = jnp.concatenate([k1[n].astype(F32) for n in range(3)] + [jnp.zeros((7, chan), F32)], axis=0)
    low = [
        jnp.concatenate([full[3 * (2 - a) + 2 - b : 3 * (2 - a) + 3 - b] for a in range(3)], axis=1)
        for b in range(3)
    ]
    rest = jnp.zeros((1, ws.shape[1] - 3 * chan), F32)
    for b in range(3):
        base = jnp.concatenate([low[b], rest], axis=1)
        many = ws.shape[0] // 3
        rolled = [pltpu.roll(base, chan * m, 1) if m else base for m in range(many)]
        ws[many * b : many * (b + 1)] = jnp.concatenate(rolled, axis=0).astype(BF16)
    store_ws = pltpu.make_async_copy(ws, ws_hbm, sems.at[7])
    store_ws.start()
    count, frame_dev = all_masks.shape[0] // 3, all_masks.shape[1]
    frames = iota((count, frame_dev), 0) * frame_dev + iota((count, frame_dev), 1)
    for n, mask in enumerate(frame_masks(bounds, frames)):
        all_masks[n * count : (n + 1) * count] = mask
    q = iota(edge_masks.shape, 0)
    lane = iota(edge_masks.shape, 1)
    k = q % 8
    frames = (q // 8) * frame_dev + jnp.where(k < 4, k, k + frame_dev - 8)
    living, behind, ahead = frame_masks(bounds, frames)
    living = jnp.where((k == 0) | (k == 7), living, 0.0)
    edge_masks[...] = jnp.where(lane == 0, living, jnp.where(lane == 1, behind, jnp.where(lane == 2, ahead, 0.0)))
    params[...] = jnp.concatenate(
        [vectors[n] for n in range(4)] + [jnp.zeros((4, chan), F32)], axis=0
    )
    tap = iota((16, 128), 0)
    lane = iota((16, 128), 1)
    i = (tap * 11) >> 5
    ninth = (lane * 57) >> 9
    to_band = (lane == BAND * (tap - 3 * i) + i) & (tap < 9)
    to_left = (ninth == tap) & (tap < 9)
    to_right = (lane - 9 * ninth == tap) & (lane < 81)
    to_single = (lane == 81 + tap) & (tap < 9)
    source = iota((128, 128), 0) - 81
    lane = iota((128, 128), 1)
    ninth = (lane * 57) >> 9
    inside = (source >= 0) & (source < 9) & (lane < 81)
    twice[...] = jnp.where(inside, (source == ninth).astype(F32) + (source == lane - 9 * ninth).astype(F32), 0.0)
    for r in range(wf.shape[0] // chan):
        at = slice(r * chan, (r + 1) * chan)
        wf[at] = (pltpu.roll(forward, 3 * chan * r, 1) if r else forward).astype(BF16)
    k1t[...] = full
    k = full.astype(BF16)
    lanes = [dot(k, select.astype(BF16), ((0,), (0,))) for select in (to_band, to_left, to_right, to_single)]
    pairs[...] = lanes[1] * lanes[2]
    singles[...] = lanes[3]
    for m in range(w1.shape[0] // chan):
        w1[m * chan : (m + 1) * chan] = (pltpu.roll(lanes[0], m, 1) if m else lanes[0]).astype(BF16)
    store_ws.wait()


def feature_rows(centre, *parts):
    def folded(v):
        return jnp.sum(halves(v), axis=0, keepdims=True)

    rows = [jnp.zeros((1, 128), F32)] * 96
    for taps, weight in parts:
        z = [tap - centre for tap in taps]
        for s in range(9):
            left = z[s] * weight
            rows[81 + s] = rows[81 + s] + folded(left)
            for t in range(s, 9):
                rows[9 * s + t] = rows[9 * t + s] = rows[9 * s + t] + folded(left * z[t])
    return to_lanes(jnp.sum(jnp.concatenate(rows, axis=0), axis=1, keepdims=True))


def summed_blocks(ref, devices, by=1):
    block = ref.shape[0] // devices
    period = max(8 // math.gcd(block, 8), by)
    step = period * block
    total = ref[0:step, :]
    for at in range(step, ref.shape[0], step):
        total = total + ref[at : at + step, :]
    results = []
    for first in range(by):
        result = total[first * block : (first + 1) * block]
        for n in range(first + by, period, by):
            result = result + total[n * block : (n + 1) * block]
        results.append(result)
    return results if by > 1 else results[0]


def moved_rows(v, step):
    if step == 0:
        return v
    count = v.shape[0]
    if abs(step) >= count:
        return jnp.zeros_like(v)
    zero = jnp.zeros((abs(step), v.shape[1]), v.dtype)
    if step > 0:
        return jnp.concatenate([zero, v[: count - step]], axis=0)
    return jnp.concatenate([v[-step:], zero], axis=0)


def silu_halves(h):
    t = jnp.tanh(h)
    one = 1.0 + t
    return h * one, one * (1.0 + h * (1.0 - t))


def forward_one(recv, spec, pairs, singles, twice, w1, wf, params, masks, all_masks, edge_masks,
                pre_two, payload, act, x3, stats, features_out, pre_one, got, strips, halo, rows_out):
    devices = recv.shape[0]
    n_mel, count = lax.axis_size("mel"), lax.axis_size("tm")
    rows = MEL_ROWS
    mels = n_mel * rows
    wide = masks.shape[1]
    frame_dev = wide - RIM
    chan = params.shape[1]
    me_m, me_t = lax.axis_index("mel"), lax.axis_index("tm")
    usable, behind, ahead = (masks[n : n + 1] for n in range(3))
    total = masks[3:4, 0:1]
    got[...] = recv[...].astype(F32).reshape(devices * FIRST, 128)

    def every(n):
        return got[pl.ds(n, devices, stride=FIRST), :]

    lane = iota((count, 128), 1)
    bands = [got[pl.ds(FIRST * k * count + COLUMNS, count, stride=FIRST), :] for k in range(n_mel)]
    for c in range(8):
        column = jnp.zeros((count, 128), F32)
        for k, band in enumerate(bands):
            part = jnp.where(lane // rows == c, band, 0.0)
            column = column + (pltpu.roll(part, rows * (k - c) % 128, 1) if k != c else part)
        strips[pl.ds(c, count, stride=8), :] = column
    at = pl.multiple_of(FIRST * (jnp.maximum(me_m - 1, 0) * count + me_t), 8)
    above = got[pl.ds(at, 16), :] * (me_m > 0).astype(F32)
    at = pl.multiple_of(FIRST * (jnp.minimum(me_m + 1, n_mel - 1) * count + me_t), 8)
    below = got[pl.ds(at, 16), :] * (me_m < n_mel - 1).astype(F32)
    above = jnp.concatenate([above[4:8], above[12:16]], axis=1)
    below = jnp.concatenate([below[0:4], below[8:12]], axis=1)
    own = spec[0].astype(F32) * usable[:, :frame_dev]
    at = pl.multiple_of(8 * jnp.minimum(me_t + 1, count - 1), 8)
    after = strips[pl.ds(at, 8), :][:, :mels] * (me_t + 1 < count).astype(F32)
    at = pl.multiple_of(8 * jnp.maximum(me_t - 1, 0), 8)
    before = strips[pl.ds(at, 8), :][:, :mels] * (me_t > 0).astype(F32)
    sides = jnp.concatenate([after[0:4], before[4:8], jnp.zeros((8, mels), F32)], axis=0).astype(BF16)
    side = iota((16, RIM), 0)
    place = iota((16, RIM), 1) == jnp.where(side < 4, side, jnp.where(side < 8, side + RIM - 8, -1))
    halo[0:8] = jnp.zeros((8, RIM), F32)
    halo[mels : mels + 8] = jnp.zeros((8, RIM), F32)
    halo[4 : mels + 4] = dot(sides, place.astype(BF16), ((0,), (0,)))
    rim = halo[pl.ds(pl.multiple_of(me_m * rows, 8), BAND), :]
    near = jnp.concatenate([jnp.concatenate([above, own, below], axis=0), rim], axis=1)
    x3[...] = jnp.concatenate(
        [
            pltpu.roll(near, 1, 1) * behind,
            near,
            pltpu.roll(near, wide - 1, 1) * ahead,
            jnp.broadcast_to(usable, (BAND, wide)),
            jnp.zeros((128 - 4 * BAND, wide), F32),
        ],
        axis=0,
    ).astype(BF16)
    pre_one[...] = dot(w1[...], x3[...])
    lane = iota((1, 128), 1)
    parts = jnp.where(lane < 92, every(SUMS) + every(SUMS + 1) + every(SUMS + 2), 0.0)
    centres, numbers = parts[:, 90:91], parts[:, 91:92]
    centre = jnp.sum(centres * numbers, axis=0, keepdims=True)
    centre = centre / jnp.maximum(jnp.sum(numbers, axis=0, keepdims=True), 1.0)
    delta = centres - centre
    features = jnp.sum(parts + delta * numbers * jnp.where(lane < 81, delta, 1.0), axis=0, keepdims=True)
    moved = jnp.sum(delta * parts, axis=0, keepdims=True)
    def edge_row(k, n):
        first = FIRST * k * count + n
        return jnp.concatenate(
            [got[pl.ds(first, count, stride=FIRST), :], got[pl.ds(first + 8, count, stride=FIRST), :]], axis=1
        )

    edge_rows = [[edge_row(k, n) for n in (0, 1, 6, 7)] for k in range(n_mel)]
    zero = jnp.zeros((count, frame_dev), F32)
    rows_of = [[], [], []]
    for k, (top, second, fore, bottom) in enumerate(edge_rows):
        for n, v in enumerate((edge_rows[k - 1][3] if k else zero, top, second)):
            rows_of[n].append(v)
        for n, v in enumerate((fore, bottom, edge_rows[k + 1][0] if k + 1 < n_mel else zero)):
            rows_of[n].append(v)
    f_usable, f_behind, f_ahead = (all_masks[n * count : (n + 1) * count, :] for n in range(3))
    lane = iota((count, frame_dev), 1)

    def frame_before(v):
        v = pltpu.roll(v, 1, 1)
        return jnp.where(lane == 0, pltpu.roll(v, 1, 0), v) * f_behind

    def frame_after(v):
        v = pltpu.roll(v, frame_dev - 1, 1)
        return jnp.where(lane == frame_dev - 1, pltpu.roll(v, count - 1, 0), v) * f_ahead

    taps = []
    for group in rows_of:
        for move in (frame_before, lambda v: v, frame_after):
            taps.append(jnp.concatenate([move(v) for v in group], axis=1))
    f_usable = jnp.concatenate([f_usable] * (2 * n_mel), axis=1)
    borders = (taps, f_usable)
    edge = strips[...]
    q_usable, q_behind, q_ahead = (edge_masks[:, n : n + 1] for n in range(3))
    lane = iota((count * 8, 128), 1)
    inside = (lane < mels) & (lane % rows != 0) & (lane % rows != rows - 1)
    shifted = [
        pltpu.roll(edge, 1, 0) * q_behind,
        edge,
        pltpu.roll(edge, count * 8 - 1, 0) * q_ahead,
    ]
    taps = [pltpu.roll(v, (1 - i) % 128, 1) if i != 1 else v for i in range(3) for v in shifted]
    features = features + feature_rows(centre, borders, (taps, jnp.where(inside, q_usable, 0.0)))
    features = jnp.where(iota((1, 128), 1) < 90, features, 0.0)
    near_mean = jnp.sum(singles[...] * features, axis=1, keepdims=True) / total
    around = jnp.sum(singles[...], axis=1, keepdims=True)
    square = jnp.sum(pairs[...] * features, axis=1, keepdims=True)
    square = (square + 2.0 * around * jnp.sum(singles[...] * moved, axis=1, keepdims=True)) / total
    inv = lax.rsqrt(square - near_mean * near_mean + 1e-05)
    mean = near_mean + centre * around
    lane = iota((chan, 128), 1)
    stats[0:chan] = jnp.where(lane == 0, mean, jnp.where(lane == 1, inv, 0.0))
    stats[chan : chan + 8] = jnp.broadcast_to(to_lanes(near_mean), (8, 128))
    stats[chan + 8 : chan + 16] = jnp.broadcast_to(to_lanes(inv), (8, 128))
    scale = 0.5 * to_column(params[0:1], chan) * inv
    shift = 0.5 * to_column(params[1:2], chan) - mean * scale
    stats[chan + 16 :] = jnp.where(lane == 0, scale, jnp.where(lane == 1, shift, 0.0))
    scale = jnp.broadcast_to(scale, (chan, wide))
    shift = jnp.broadcast_to(shift, (chan, wide))
    ext = w1.shape[0] // chan
    block, taps = wf.shape
    first = jnp.zeros((chan, 128), F32)
    second = jnp.zeros((chan, 128), F32)
    own_mask = usable[:, :frame_dev]
    low_masks = [m.astype(BF16) for m in (usable, behind, ahead)]
    for r in range(ext):
        value, _ = silu_halves(pre_one[r * chan : (r + 1) * chan, :] * scale + shift)
        if not 0 <= r - 3 < rows:
            value = value * row_valid(r - 3, rows)
        base = r * 3 * chan
        low = value.astype(BF16) * low_masks[0]
        act[base : base + chan, :], act[base + 2 * chan : base + 3 * chan, :] = shifted_frames(low, *low_masks[1:])
        act[base + chan : base + 2 * chan, :] = low
        if r < 3 or r % 2 == 0:
            continue
        g = (r - 3) // 2
        result = dot(wf[...], act[g * 3 * block : g * 3 * block + taps, :frame_dev])
        pre_two[g * block : (g + 1) * block, :frame_dev] = result
        if g % 2:
            beside = [act[n * 3 * block : n * 3 * block + taps, frame_dev:] for n in (g - 1, g)]
            beside = dot(wf[...], jnp.concatenate(beside, axis=1))
            for n in range(2):
                pre_two[(g - 1 + n) * block : (g + n) * block, frame_dev:] = beside[:, n * RIM : (n + 1) * RIM]
        for q in range(2):
            if 2 <= 2 * g + q < rows + 2:
                p = result[q * chan : (q + 1) * chan]
                masked = p * own_mask
                first = first + halves(masked)
                second = second + halves(masked * p)
    moved = dot(jnp.broadcast_to(moved, (8, 128)), twice[...], precision=EXACT)[0:1]
    features_out[...] = jnp.concatenate(
        [features + moved, jnp.broadcast_to(centre, (1, 128)), jnp.zeros((6, 128), F32)], axis=0
    )
    share = share_of(devices, chan)

    def put(n, value):
        rows_out[pl.ds(n, devices, stride=SECOND), :] = jnp.broadcast_to(value, (devices, 128))

    for n in range(share):
        put(3 + n, moved_rows(every(EDGES + share + n), count))
        put(3 + share + n, moved_rows(every(EDGES + n), -count))
    for n in [0, 1, 2] + list(range(3 + 2 * share, SECOND - 1)):
        put(n, jnp.zeros((1, 128), F32))
    lane = iota((devices, 128), 1)
    tm = iota((devices, 128), 0) % count
    lefts = jnp.where(lane >= SIDE, every(SUMS), 0.0)
    rights = jnp.where(lane >= SIDE, every(SUMS + 1), 0.0)
    beside = jnp.zeros((devices, 128), F32)
    for n, step in enumerate((0, count, -count)):
        one = jnp.where(tm > 0, moved_rows(rights, step + 1), 0.0)
        two = jnp.where(tm < count - 1, moved_rows(lefts, step - 1), 0.0)
        beside = beside + pltpu.roll(one, (32 * n - SIDE) % 128, 1) + pltpu.roll(two, (32 * n + 16 - SIDE) % 128, 1)
    put(SECOND - 1, beside)
    first = jnp.sum(first, axis=1, keepdims=True)
    second = jnp.sum(second, axis=1, keepdims=True)
    parts = list(three_parts(to_lanes(first) + to_lanes(second, chan)))
    parts = jnp.concatenate(parts + [jnp.zeros((SECOND - 3, 128), F32)], axis=0)
    for d in range(devices):
        payload[d] = (rows_out[SECOND * d : SECOND * (d + 1), :] + parts).astype(BF16)


def spreading(half):
    lane = iota((half, 2 * half), 1)
    return jnp.where(lane >> 1 == iota((half, 2 * half), 0), 0.25, 0.0).astype(BF16)


def half_share(devices, taps):
    return -(-taps // 2 // devices)


def backward_scaled(recv, pre_two, act, own_rows, params, masks,
                    grad, kept_half, sent_half, totals, stats, up, right, got, halved):
    devices = recv.shape[0]
    got[...] = recv[:, 0:SECOND, :].astype(F32).reshape(devices * SECOND, 128)
    chan = params.shape[1]
    half = own_rows.shape[1]
    frame_dev = 2 * half
    rows = MEL_ROWS
    up[...] = dot(own_rows[...], spreading(half))
    usable = masks[0:1, :frame_dev]
    total = masks[3:4, 0:1]
    sums = [got[pl.ds(n, devices, stride=SECOND), :] for n in range(3)]
    sums = jnp.sum(sums[0] + sums[1] + sums[2], axis=0, keepdims=True)
    mean = to_column(sums, chan) / total
    inv = lax.rsqrt(to_column(sums, chan, chan) / total - mean * mean + 1e-05)
    scale = 0.5 * to_column(params[2:3], chan) * inv
    shift = 0.5 * to_column(params[3:4], chan) - mean * scale
    lane = iota((chan, 128), 1)
    columns = jnp.zeros((chan, 128), F32)
    for n, column in enumerate((mean, inv, scale, shift)):
        columns = jnp.where(lane == n, column, columns)
    stats[0:chan] = columns
    stats[chan : chan + 8] = jnp.broadcast_to(to_lanes(inv), (8, 128))
    mean, inv, scale, shift = (jnp.broadcast_to(v, (chan, frame_dev)) for v in (mean, inv, scale, shift))
    first = jnp.zeros((chan, 128), F32)
    second = jnp.zeros((chan, 128), F32)
    mask = 0.5 * usable
    right[3 * chan :] = jnp.ones((16, rows * frame_dev), BF16)
    table = jnp.zeros((9 * chan, 3 * chan + 16), F32)
    for m in range(rows):
        at = slice(m * chan, (m + 1) * chan)
        pre = pre_two[(m + 2) * chan : (m + 3) * chan, :frame_dev]
        _, slope = silu_halves(pre * scale + shift)
        g = up[m // 2 * chan : (m // 2 + 1) * chan, :] * slope * mask
        grad[at, :] = g
        normed = (pre - mean) * inv
        first = first + halves(g * normed)
        second = second + halves(g)
        lanes = slice(m * frame_dev, (m + 1) * frame_dev)
        right[0:chan, lanes] = g.astype(BF16)
        right[chan : 2 * chan, lanes] = normed.astype(BF16)
        right[2 * chan : 3 * chan, lanes] = (g - right[0:chan, lanes].astype(F32)).astype(BF16)
        if m in (5, 11, rows - 1):
            start = m - m % 6
            left = [act[(n + 2) * 3 * chan : (n + 5) * 3 * chan, :frame_dev] for n in range(start, m + 1)]
            lanes = slice(start * frame_dev, (m + 1) * frame_dev)
            table = table + dot(jnp.concatenate(left, axis=1), right[:, lanes], ((1,), (1,)))
    first = jnp.sum(first, axis=1, keepdims=True)
    second = jnp.sum(second, axis=1, keepdims=True)
    totals[...] = jnp.broadcast_to(to_lanes(first) + to_lanes(second, chan), (8, 128))
    rest = jnp.concatenate([table[:, 2 * chan :], jnp.zeros((9 * chan, chan - 16), F32)], axis=1)
    both = table[:, : 2 * chan] + jnp.where(iota(rest.shape, 1) < chan, rest, 0.0)
    single = rest[:, chan : chan + 1]
    taps = 9 * chan // 2
    lane = iota((devices, 128), 1)
    for h in range(2):
        halved[h, 0:taps] = both[h * taps : (h + 1) * taps]
        constants = jnp.zeros((devices, 128), F32)
        for k in range(half_share(devices, 9 * chan)):
            at = h * taps + k * devices
            ones = single[at : min(at + devices, (h + 1) * taps)]
            if ones.shape[0] < devices:
                ones = jnp.concatenate([ones, jnp.zeros((devices - ones.shape[0], 1), F32)], axis=0)
            constants = jnp.where(lane == k, ones, constants)
        halved[h, taps:] = constants
    core = lax.axis_index("tm") % 2
    kept_half[...] = halved[core]
    sent_half[...] = halved[1 - core]


def around(recv, pre_two, masks, stats, ring, rim, pairs, sides, up, got, beyond):
    devices = recv.shape[0]
    got[...] = recv[:, 0:SECOND, :].astype(F32).reshape(devices * SECOND, 128)
    rows = MEL_ROWS
    many = rows // 2
    wide = pre_two.shape[1]
    frame_dev = wide - RIM
    chan = pre_two.shape[0] // (rows + 4)
    usable = masks[0:1]
    share = share_of(devices, chan)
    holders = chan // share

    def every(n):
        return got[pl.ds(n, devices, stride=SECOND), :]

    beside = every(SECOND - 1)[:holders]
    lane = iota((holders, RIM), 1)
    for n in range(share):
        first = n * holders
        beyond[first : first + holders, :] = every(3 + n)[:holders]
        beyond[chan + first : chan + first + holders, :] = every(3 + share + n)[:holders]
        for r in range(many + 2):
            at = many * n + (r if r < many else 32 + many - 1 if r == many else 64)
            left, right_of = beside[:, at : at + 1], beside[:, at + 16 : at + 17]
            side = jnp.where(lane >= RIM - 2, 0.25 * left, jnp.where(lane < 2, 0.25 * right_of, 0.0))
            sides[r * chan + first : r * chan + first + holders, :] = side
    up[...] = dot(beyond[...].astype(BF16), spreading(frame_dev // 2))
    scale = jnp.broadcast_to(stats[0:chan, 2:3], (chan, wide))
    shift = jnp.broadcast_to(stats[0:chan, 3:4], (chan, wide))
    for n, m in enumerate((-2, -1, rows, rows + 1)):
        below = n // 2
        upstream = jnp.concatenate(
            [
                up[below * chan : (below + 1) * chan, :],
                sides[(many + below) * chan : (many + below + 1) * chan, :],
            ],
            axis=1,
        )
        _, slope = silu_halves(pre_two[(m + 2) * chan : (m + 3) * chan, :] * scale + shift)
        ring[n * chan : (n + 1) * chan, :] = upstream * slope * (usable * (0.5 * row_valid(m, rows)))
    both = None
    for m in range(rows):
        at = slice((m + 2) * chan, (m + 3) * chan)
        _, slope = silu_halves(pre_two[at, frame_dev:] * scale[:, frame_dev:] + shift[:, frame_dev:])
        upstream = sides[m // 2 * chan : (m // 2 + 1) * chan, :]
        rim[m * chan : (m + 1) * chan, :] = upstream * slope * (0.5 * usable[:, frame_dev:])
        value, _ = silu_halves(pre_two[at, :frame_dev] * scale[:, :frame_dev] + shift[:, :frame_dev])
        value = value * usable[:, :frame_dev]
        both = value if m % 2 == 0 else both + value
        if m % 2:
            pairs[m // 2 * chan : (m // 2 + 1) * chan, :] = both


def pack_sums(kept_half, received, totals, after, payload):
    del after
    devices = kept_half.shape[0] - TAPS // 2
    block = payload.shape[0] // devices
    payload[pl.ds(0, devices, stride=block), :] = jnp.broadcast_to(totals[0:1], (devices, 128))
    taps = TAPS // 2
    total = kept_half[...] + received[...]
    for k in range(block - 2):
        cut = total[k * devices : min((k + 1) * devices, taps)]
        if cut.shape[0] < devices:
            cut = jnp.concatenate([cut, jnp.zeros((devices - cut.shape[0], 128), F32)], axis=0)
        payload[pl.ds(1 + k, devices, stride=block), :] = cut
    payload[pl.ds(block - 1, devices, stride=block), :] = total[taps:]


def pool(totals, pairs, out, gain_out, bias_out, temp):
    gain_out[...] = totals[0:1, : gain_out.shape[1]]
    bias_out[...] = totals[0:1, gain_out.shape[1] :]
    chan, rows, half = out.shape[1:]
    to_mean = jnp.where(iota((2 * half, half), 0) >> 1 == iota((2 * half, half), 1), 0.25, 0.0)
    pooled = dot(pairs[...], to_mean, precision=EXACT)
    for r in range(rows):
        temp[pl.ds(r, chan, stride=rows), :] = pooled[r * chan : (r + 1) * chan]
    out[0] = temp[...].reshape(chan, rows, half).astype(BF16)


def backward(recv, pre_two, grad, ring, rim, stats_two, w1, x3, stats, params, masks, wb,
             out, own_low, payload, totals, g3, pre_one, g1):
    chan = params.shape[1]
    rows = MEL_ROWS
    wide = pre_two.shape[1]
    frame_dev = wide - RIM
    usable = masks[0:1]
    behind, ahead = (masks[n : n + 1].astype(BF16) for n in (1, 2))
    total = masks[3:4, 0:1]
    devices = payload.shape[0] // 14
    pre_one[...] = dot(w1[3 * chan : (rows + 3) * chan], x3[:, :frame_dev])

    even, odd = summed_blocks(recv, devices, 2)
    sums = even[0:1] + odd[0:1]
    gain_sum, bias_sum = sums[:, :chan], sums[:, chan:]
    totals[...] = jnp.broadcast_to(sums, (8, 128))
    mean, inv = stats_two[0:chan, 0:1], stats_two[0:chan, 1:2]
    factor = to_column(params[2:3], chan) * inv
    gain_part = factor * (to_column(sums, chan) / total * inv)
    bias_part = factor * (to_column(sums, chan, chan) / total) - mean * gain_part
    gain_part = jnp.broadcast_to(gain_part, (chan, wide))
    bias_part = jnp.broadcast_to(bias_part, (chan, wide))
    factor = jnp.broadcast_to(factor, (chan, wide))
    scale = jnp.broadcast_to(stats[chan + 16 :, 0:1], (chan, frame_dev))
    shift = jnp.broadcast_to(stats[chan + 16 :, 1:2], (chan, frame_dev))
    factor_one = jnp.broadcast_to(to_column(params[0:1], chan) * stats[0:chan, 1:2], (chan, frame_dev))
    own_mask = 0.5 * usable[:, :frame_dev]
    count = pre_two.shape[0] // chan
    share = even.shape[0] - 2
    mine = jnp.concatenate([even[1 : share + 1], odd[1 : share + 1]], axis=0)
    single = jnp.concatenate([to_column(v[share + 1 :], share) for v in (even, odd)], axis=0)
    factor_l = params[2:3] * stats_two[chan : chan + 1, :chan]
    mine = mine[:, :chan] - (bias_sum * single + gain_sum * mine[:, chan:]) / total
    mine = factor_l * mine
    mine = jnp.concatenate([mine[:share], mine[share:]], axis=1)
    if share < 9:
        mine = jnp.concatenate([mine, jnp.zeros((9 - share, 128), F32)], axis=0)
    table = jnp.zeros((chan, 128), F32)

    def tap_sums(m):
        part = g1[m * chan : (m + 4) * chan, :]
        high = lax.reduce_precision(part, 8, 7)
        low = (part - high).astype(BF16)
        taps_in = x3[:, :frame_dev]
        products = dot(high.astype(BF16), taps_in, ((1,), (1,))) + dot(low, taps_in, ((1,), (1,)))
        moved = [pltpu.roll(products[k * chan : (k + 1) * chan], 128 - (m + k + 3), 1) for k in range(4)]
        return (moved[0] + moved[1]) + (moved[2] + moved[3])

    for q in range(count):
        at = slice(q * chan, (q + 1) * chan)
        mask = usable if 0 <= q - 2 < rows else usable * row_valid(q - 2, rows)
        if 2 <= q < rows + 2:
            own = slice((q - 2) * chan, (q - 1) * chan)
            scaled = jnp.concatenate([grad[own, :], rim[own, :]], axis=1)
        else:
            n = q if q < 2 else q - rows
            scaled = ring[n * chan : (n + 1) * chan, :]
        low = (factor * scaled - (bias_part + pre_two[at, :] * gain_part) * mask).astype(BF16)
        out[at, :] = low
        if not 1 <= q < count - 1:
            continue
        base = (q - 1) * 3 * chan
        for n, v in enumerate((low,) + shifted_frames(low, behind, ahead)):
            spot = base + (1, 0, 2)[n] * chan
            g3[spot : spot + chan, :] = v[:, :frame_dev]
        start = q - 4
        if start < 0 or start % 2:
            continue
        result = dot(wb[...], g3[start * 3 * chan : (start + 4) * 3 * chan, :])
        for n in range(2):
            m = start + n
            at = slice(m * chan, (m + 1) * chan)
            _, slope = silu_halves(pre_one[at, :] * scale + shift)
            value = result[n * chan : (n + 1) * chan] * slope * own_mask
            own_low[at, :] = (value * factor_one).astype(BF16)
            g1[at, :] = value
        if start % 4 == 2 and start > 2:
            table = table + tap_sums(start - 6)
    table = table + tap_sums(rows - 4)
    table = table.T
    places = [BAND * j + i for i in range(3) for j in range(3)] + [3 * BAND]
    rows10 = jnp.concatenate([table[n : n + 1] for n in places], axis=0)
    sums = jnp.concatenate([rows10[0:5], rows10[5:10]], axis=1)
    block = jnp.concatenate([sums, mine], axis=0)
    block = jnp.concatenate([block] * 4, axis=0)
    for d in range(0, devices, 4):
        payload[14 * d : 14 * (d + 4), :] = block


def transposed(grad, own_low, w1, wb, x3, stats, features, k1t, params, masks, ws_hbm,
               first, ws, normed_taps, low, g3, rim, sem):
    load = pltpu.make_async_copy(ws_hbm, ws, sem)
    load.start()
    rows = MEL_ROWS
    chan = own_low.shape[0] // rows
    wide = grad.shape[1]
    frame_dev = wide - RIM
    count = grad.shape[0] // chan
    usable = masks[0:1]
    behind, ahead = (masks[n : n + 1].astype(BF16) for n in (1, 2))
    scale = jnp.broadcast_to(stats[chan + 16 :, 0:1], (chan, wide))
    shift = jnp.broadcast_to(stats[chan + 16 :, 1:2], (chan, wide))
    factor = jnp.broadcast_to(to_column(params[0:1], chan) * stats[0:chan, 1:2], (chan, wide))
    edge = (0, 1, 2, 3, count - 4, count - 3, count - 2, count - 1)
    for q in range(count):
        value = grad[q * chan : (q + 1) * chan, :]
        for n, v in enumerate((value,) + shifted_frames(value, behind, ahead)):
            spot = (3 * q + (1, 0, 2)[n]) * chan
            rim[spot : spot + chan, :] = v[:, frame_dev:]
            if q in edge:
                spot = (3 * edge.index(q) + (1, 0, 2)[n]) * chan
                g3[spot : spot + chan, :] = v[:, :frame_dev]
    low[chan : (rows + 1) * chan, :frame_dev] = own_low[...]

    def put(m, lanes, result, pre_one):
        at = slice((m + 1) * chan, (m + 2) * chan)
        _, slope = silu_halves(pre_one * scale[:, lanes] + shift[:, lanes])
        mask = usable[:, lanes] * (0.5 * row_valid(m, rows))
        low[at, lanes] = (result * slope * mask * factor[:, lanes]).astype(BF16)

    pre_one = dot(w1[2 * chan : (rows + 4) * chan, :], x3[:, frame_dev:])
    beside = slice(frame_dev, wide)
    for start in range(0, rows + 2, 2):
        result = dot(wb[...], rim[start * 3 * chan : (start + 4) * 3 * chan, :])
        for n in range(2):
            at = slice((start + n) * chan, (start + n + 1) * chan)
            put(start + n - 1, beside, result[n * chan : (n + 1) * chan], pre_one[at])
    own = slice(0, frame_dev)
    result = dot(wb[...], g3[: 4 * 3 * chan, :])
    put(-1, own, result[:chan], dot(w1[2 * chan : 3 * chan, :], x3[:, :frame_dev]))
    result = dot(wb[...], g3[4 * 3 * chan :, :])
    put(rows, own, result[chan:], dot(w1[(rows + 3) * chan : (rows + 4) * chan, :], x3[:, :frame_dev]))
    row = features[0:1, :]
    lane = iota((1, 128), 1)
    gram = jnp.concatenate(
        [jnp.where(lane < 9, pltpu.roll(row, 128 - 9 * t, 1) if t else row, 0.0) for t in range(9)]
        + [jnp.zeros((7, 128), F32)],
        axis=0,
    )
    single = to_column(row, 16, 81)[0:9]
    k_rows = jnp.concatenate([k1t[...], jnp.zeros((112, chan), F32)], axis=0)
    mean_l, inv_l = stats[chan : chan + 1, :chan], stats[chan + 8 : chan + 9, :chan]
    normed = inv_l * (dot(gram, k_rows, precision=EXACT)[0:9] - single * mean_l)
    normed_taps[0:16] = jnp.concatenate([normed, jnp.zeros((7, chan), F32)], axis=0)
    normed_taps[16:32] = jnp.broadcast_to(to_column(row, 16, 81), (16, chan))
    load.wait()
    first[...] = dot(ws[...], low[...])


def finish(recv, features, stats, k1t, first, ws, w1, x3, normed_taps, params, masks,
           spec_hbm, kernel_one_hbm, kernel_two_hbm, gain_hbm, bias_hbm,
           spec_grad, kernel_one, kernel_two, gain_out, bias_out, sems):
    chan = params.shape[1]
    rows = MEL_ROWS
    wide = x3.shape[1]
    frame_dev = wide - RIM
    usable, behind, ahead = (masks[n : n + 1] for n in range(3))
    total = masks[3:4, 0:1]
    gain = params[0:1]
    count = recv.shape[0] // 14
    share = half_share(count, 9 * chan)
    sums = summed_blocks(recv, count)[0:5]
    ten = jnp.concatenate([sums[:, :chan], sums[:, chan:]], axis=0)
    bias_sum = ten[9:10]
    mean_l, inv_l = stats[chan : chan + 1, :chan], stats[chan + 8 : chan + 9, :chan]
    ten = ten - features[1:2, 0:1] * bias_sum
    k = k1t[0:9]
    gain_sum = inv_l * (jnp.sum(k * ten[0:9], axis=0, keepdims=True) - mean_l * bias_sum)
    gain_out[...] = gain_sum
    bias_out[...] = bias_sum
    factor_l = gain * inv_l
    scale = factor_l * gain_sum / total * inv_l
    scale = jnp.concatenate(
        [scale * row_valid(-1, rows)] + [scale] * rows + [scale * row_valid(rows, rows)], axis=1
    )
    many = 3 * rows

    def in_parts(v, right):
        high = lax.reduce_precision(v, 8, 7)
        v = dot(jnp.concatenate([high, v - high], axis=0).astype(BF16), right)
        return v[:many] + v[many:]

    combined = in_parts(ws[...].astype(F32) * scale, w1[2 * chan : (rows + 4) * chan, :])
    left = [recv[pl.ds(5 + p, count, stride=14), :] for p in range(share)]
    taps = TAPS // 2
    whole = [jnp.concatenate([v[:, h * chan : (h + 1) * chan] for v in left], axis=0)[:taps] for h in range(2)]
    whole = jnp.concatenate(whole, axis=0)
    for t in range(9):
        kernel_two[t] = whole[t * chan : (t + 1) * chan].T
    stores = [pltpu.make_async_copy(kernel_two, kernel_two_hbm, sems.at[4])]
    stores[0].start()
    taken = in_parts(combined, x3[...])
    taps = first[...] - taken
    moved = [taps[rows * b : rows * (b + 1)] for b in range(3)]
    mean_full = mean_l + features[1:2, 0:1] * jnp.sum(k, axis=0, keepdims=True)
    constant = jnp.sum(k * (factor_l * (bias_sum - gain_sum * inv_l * mean_full) / total), axis=1, keepdims=True)
    for a in range(3):
        row = iota((rows, 1), 0) + (a - 1) + lax.axis_index("mel") * rows
        valid = ((row >= 0) & (row < lax.axis_size("mel") * rows)).astype(F32) * usable
        for b in range(3):
            t = 3 * (2 - a) + 2 - b
            moved[b] = moved[b] - constant[t : t + 1] * valid
    result = pltpu.roll(moved[0], 1, 1) * behind + moved[1] + pltpu.roll(moved[2], wide - 1, 1) * ahead
    spec_grad[0] = (result * usable)[:, :frame_dev]
    grad_taps = factor_l * (ten[0:9] - (bias_sum * normed_taps[16:25] + gain_sum * normed_taps[0:9]) / total)
    for i in range(3):
        kernel_one[i] = grad_taps[3 * i : 3 * i + 3]
    outs = ((spec_grad, spec_hbm), (kernel_one, kernel_one_hbm), (gain_out, gain_hbm), (bias_out, bias_hbm))
    wait_all(stores + start_all(*outs, sems=sems))


def run(kernel, outs, scratch, *args, hbm=0, apart=(), flops=10**8, size=4 * 10**6):
    vmem = pl.BlockSpec(memory_space=pltpu.VMEM)
    devices = lax.axis_size("mel") * lax.axis_size("tm")
    specs = []
    args = list(args)
    for n, a in enumerate(args):
        if hbm and n >= len(args) - hbm:
            specs.append(pl.BlockSpec(memory_space=pltpu.HBM))
            args[n] = pltpu.with_memory_space_constraint(a, pltpu.HBM)
        else:
            specs.append(vmem)
            args[n] = pltpu.with_memory_space_constraint(a, pltpu.VMEM)
    return pl.pallas_call(
        kernel,
        out_shape=outs,
        in_specs=specs,
        out_specs=[pl.BlockSpec(memory_space=pltpu.HBM) if n in apart else vmem for n in range(len(outs))],
        scratch_shapes=scratch,
        compiler_params=pltpu.CompilerParams(vmem_limit_bytes=(29 + devices // 32) * 2**20),
        cost_estimate=pl.CostEstimate(flops=flops, bytes_accessed=size, transcendentals=0),
    )(*args)


def shape(dims, dtype=F32):
    return jax.ShapeDtypeStruct(dims, dtype)


def kept(dims, dtype=F32):
    return pltpu.VMEM(dims, dtype)


def far(dims, dtype=F32):
    return pltpu.HBM(dims, dtype)


def exchange(blocks, axes=AXES):
    return lax.all_to_all(blocks, axes, 0, 0, tiled=True)


def exchange_rows(rows, axes=AXES):
    return exchange(rows[:, None, :], axes)[:, 0, :]


def shards(spectrum, clip_bounds, kernel_one, gain_one, bias_one, kernel_two, gain_two, bias_two, pooled_grad):
    _, rows, frame_dev = spectrum.shape
    chan = kernel_two.shape[0]
    n_mel, n_tm = lax.axis_size("mel"), lax.axis_size("tm")
    devices = n_mel * n_tm
    half = frame_dev // 2
    wide = frame_dev + RIM
    mels = n_mel * rows

    packed, own, spec, masks = run(
        pack,
        [
            kept((devices, FIRST, 128), BF16),
            kept(pooled_grad.shape, BF16),
            kept(spectrum.shape, BF16),
            kept((8, wide)),
        ],
        [
            pltpu.SMEM(clip_bounds.shape, jnp.int32),
            pltpu.VMEM((2 * chan, half), F32),
            pltpu.VMEM((devices * FIRST, 128), F32),
            pltpu.SemaphoreType.DMA((3,)),
        ],
        spectrum,
        pooled_grad,
        clip_bounds,
        hbm=3,
    )
    recv = exchange(packed)
    ext = rows + 6
    span = 4 * 3 * chan
    wf, wb, w1, ws, pairs, singles, k1t, params, all_masks, edge_masks, twice, own_rows = run(
        weights,
        [
            kept((2 * chan, span), BF16),
            kept((2 * chan, span), BF16),
            kept((ext * chan, 128), BF16),
            far((rows * 3, (rows + 2) * chan), BF16),
            kept((chan, 128)),
            kept((chan, 128)),
            kept((16, chan)),
            kept((8, chan)),
            kept((3 * n_tm, frame_dev)),
            kept((n_tm * 8, 128)),
            kept((128, 128)),
            kept((chan * rows // 2, half), BF16),
        ],
        [
            pltpu.VMEM((9, chan, chan), BF16),
            pltpu.VMEM((3, 3, chan), BF16),
            pltpu.VMEM((4, 1, chan), F32),
            pltpu.SMEM(clip_bounds.shape, jnp.int32),
            pltpu.VMEM((rows * 3, (rows + 2) * chan), BF16),
            pltpu.VMEM((chan * rows // 2, half), F32),
            pltpu.SemaphoreType.DMA((8,)),
        ],
        own,
        clip_bounds,
        jnp.transpose(kernel_two, (2, 3, 0, 1)).reshape(9, chan, chan),
        jnp.transpose(kernel_one, (1, 2, 0)),
        gain_one[None],
        bias_one[None],
        gain_two[None],
        bias_two[None],
        hbm=7,
        apart=(3,),
    )
    pre_two, payload, act, x3, stats_one, features = run(
        forward_one,
        [
            kept(((rows + 4) * chan, wide)),
            kept((devices, SECOND, 128), BF16),
            kept((ext * 3 * chan, wide), BF16),
            kept((128, wide), BF16),
            kept((2 * chan + 16, 128)),
            kept((8, 128)),
        ],
        [
            pltpu.VMEM((ext * chan, wide), F32),
            pltpu.VMEM((devices * FIRST, 128), F32),
            pltpu.VMEM((n_tm * 8, 128), F32),
            pltpu.VMEM((mels + 8, RIM), F32),
            pltpu.VMEM((devices * SECOND, 128), F32),
        ],
        recv,
        spec,
        pairs,
        singles,
        twice,
        w1,
        wf,
        params,
        masks,
        all_masks,
        edge_masks,
    )
    recv = exchange(payload)
    grad, kept_half, sent_half, totals, stats_two = run(
        backward_scaled,
        [
            kept((rows * chan, frame_dev)),
            kept((TAPS // 2 + devices, 128)),
            kept((TAPS // 2 + devices, 128)),
            kept((8, 128)),
            kept((chan + 8, 128)),
        ],
        [
            pltpu.VMEM((rows // 2 * chan, frame_dev), F32),
            pltpu.VMEM((3 * chan + 16, rows * frame_dev), BF16),
            pltpu.VMEM((devices * SECOND, 128), F32),
            pltpu.VMEM((2, TAPS // 2 + devices, 128), F32),
        ],
        recv,
        pre_two,
        act,
        own_rows,
        params,
        masks,
    )
    received = lax.ppermute(sent_half, "tm", [(i, i ^ 1) for i in range(n_tm)])
    ring, rim, row_pairs = run(
        around,
        [kept((4 * chan, wide)), kept((rows * chan, RIM)), kept((rows // 2 * chan, frame_dev))],
        [
            pltpu.VMEM(((rows // 2 + 2) * chan, RIM), F32),
            pltpu.VMEM((2 * chan, frame_dev), F32),
            pltpu.VMEM((devices * SECOND, 128), F32),
            pltpu.VMEM((2 * chan, half), F32),
        ],
        recv,
        pre_two,
        masks,
        stats_two,
    )
    (payload,) = run(
        pack_sums,
        [kept((devices * (half_share(devices, 9 * chan) + 2), 128))],
        [],
        kept_half,
        received,
        totals,
        rim,
    )
    recv = exchange_rows(payload)
    grad, own_low, payload, totals = run(
        backward,
        [
            kept(((rows + 4) * chan, wide), BF16),
            kept((rows * chan, frame_dev), BF16),
            kept((devices * 14, 128)),
            kept((8, 128)),
        ],
        [
            pltpu.VMEM(((rows + 2) * 3 * chan, frame_dev), BF16),
            pltpu.VMEM((rows * chan, frame_dev), F32),
            pltpu.VMEM((rows * chan, frame_dev), F32),
        ],
        recv,
        pre_two,
        grad,
        ring,
        rim,
        stats_two,
        w1,
        x3,
        stats_one,
        params,
        masks,
        wb,
    )
    recv = exchange_rows(payload)
    pooled, gain_two_grad, bias_two_grad = run(
        pool,
        [shape((1, chan, rows // 2, half), BF16), shape((1, chan)), shape((1, chan))],
        [
            pltpu.VMEM((rows // 2 * chan, 128), F32),
        ],
        totals,
        row_pairs,
    )
    first, ws, normed_taps = run(
        transposed,
        [
            kept((rows * 3, wide)),
            kept((rows * 3, (rows + 2) * chan), BF16),
            kept((32, chan)),
        ],
        [
            pltpu.VMEM(((rows + 2) * chan, wide), BF16),
            pltpu.VMEM((8 * 3 * chan, frame_dev), BF16),
            pltpu.VMEM(((rows + 4) * 3 * chan, RIM), BF16),
            pltpu.SemaphoreType.DMA,
        ],
        grad,
        own_low,
        w1,
        wb,
        x3,
        stats_one,
        features,
        k1t,
        params,
        masks,
        ws,
        hbm=1,
    )
    spec_grad, kernel_one_grad, kernel_two_grad, gain_one_grad, bias_one_grad = run(
        finish,
        [
            shape((1, rows, frame_dev)),
            shape((3, 3, chan)),
            shape((9, chan, chan)),
            shape((1, chan)),
            shape((1, chan)),
        ],
        [
            pltpu.VMEM((1, rows, frame_dev), F32),
            pltpu.VMEM((3, 3, chan), F32),
            pltpu.VMEM((9, chan, chan), F32),
            pltpu.VMEM((1, chan), F32),
            pltpu.VMEM((1, chan), F32),
            pltpu.SemaphoreType.DMA((5,)),
        ],
        recv,
        features,
        stats_one,
        k1t,
        first,
        ws,
        w1,
        x3,
        normed_taps,
        params,
        masks,
        apart=range(5),
    )
    kernel_two_grad = jnp.transpose(kernel_two_grad.reshape(3, 3, chan, chan), (2, 3, 0, 1))
    return (
        pooled,
        spec_grad,
        jnp.transpose(kernel_one_grad, (2, 0, 1)),
        gain_one_grad[0],
        bias_one_grad[0],
        kernel_two_grad,
        gain_two_grad[0],
        bias_two_grad[0],
    )


def solution(mesh):
    return jax.shard_map(
        shards,
        mesh=mesh,
        in_specs=(
            P(None, "mel", "tm"),
            P(),
            P(),
            P(),
            P(),
            P(),
            P(),
            P(),
            P(None, None, "mel", "tm"),
        ),
        out_specs=(P(None, None, "mel", "tm"), P(None, "mel", "tm"), P(), P(), P(), P(), P(), P()),
        check_vma=False,
    )
```

```python
import math

import jax
import jax.numpy as jnp
from jax import lax
from jax.experimental import pallas as pl
from jax.experimental.pallas import tpu as pltpu
from jax.sharding import PartitionSpec as P

F32 = jnp.float32
BF16 = jnp.bfloat16
AXES = ("mel", "tm")
EXACT = lax.Precision.HIGHEST
RIM = 128
BAND = 24
MEL_ROWS = 16
FIRST = 24
SUMS, EDGES, COLUMNS = 16, 19, 23
SIDE = 96
TAPS = 576
SECOND = 8


def iota(shape, dim):
    return lax.broadcasted_iota(jnp.int32, shape, dim)


def dot(a, b, over=((1,), (0,)), precision=None):
    return lax.dot_general(a, b, (over, ((), ())), precision=precision, preferred_element_type=F32)


def to_column(lanes, count, start=0):
    shape = (count, lanes.shape[1])
    return jnp.sum(jnp.where(iota(shape, 1) == iota(shape, 0) + start, lanes, 0.0), axis=1, keepdims=True)


def to_lanes(column, start=0, width=128):
    shape = (column.shape[0], width)
    return jnp.sum(jnp.where(iota(shape, 1) == iota(shape, 0) + start, column, 0.0), axis=0, keepdims=True)


def halves(v):
    total = v[:, :128]
    for n in range(128, v.shape[1], 128):
        total = total + v[:, n : n + 128]
    return total


def frame_masks(bounds, frames):
    last = bounds.shape[1] - 1

    def living(f):
        return (f >= 0) & (f < bounds[0, last])

    def paired(f):
        both = living(f) & living(f + 1)
        for k in range(1, last):
            both = both & (f + 1 != bounds[0, k])
        return both

    return tuple(m.astype(F32) for m in (living(frames), paired(frames - 1), paired(frames)))


def row_valid(row, rows):
    mel = lax.axis_index("mel") * rows + row
    return ((mel >= 0) & (mel < lax.axis_size("mel") * rows)).astype(F32)


def start_all(*pairs, sems):
    copies = [pltpu.make_async_copy(src, dst, sems.at[n]) for n, (src, dst) in enumerate(pairs)]
    for copy in copies:
        copy.start()
    return copies


def wait_all(copies):
    for copy in copies:
        copy.wait()


def shifted_frames(value, behind, ahead):
    wide = value.shape[1]
    return pltpu.roll(value, 1, 1) * behind, pltpu.roll(value, wide - 1, 1) * ahead


def three_parts(v):
    high = lax.reduce_precision(v, 8, 7)
    mid = lax.reduce_precision(v - high, 8, 7)
    return high, mid, v - high - mid


def share_of(devices, chan):
    return -(-chan // devices)


def pack(spec_hbm, grad_hbm, bounds_hbm, out, own, spec, masks, bounds, edges, rows_out, sems):
    copies = start_all((bounds_hbm, bounds), (spec_hbm, spec), (grad_hbm, own), sems=sems)
    copies[0].wait()
    wide = masks.shape[1]
    frame_dev = wide - RIM
    devices = out.shape[0]
    rows = MEL_ROWS
    lane = iota((1, wide), 1)
    frames = lax.axis_index("tm") * frame_dev + jnp.where(lane < frame_dev + RIM // 2, lane, lane - wide)
    last = bounds.shape[1] - 1
    pixels = (bounds[0, last] * (lax.axis_size("mel") * rows)).astype(F32)
    found = frame_masks(bounds, frames)
    masks[...] = jnp.concatenate(
        list(found) + [jnp.full((1, wide), 1.0) * pixels, jnp.zeros((4, wide), F32)], axis=0
    )
    usable, behind, ahead = (m[:, :frame_dev] for m in found)
    copies[1].wait()
    x = spec[0].astype(F32) * usable
    lane = iota((1, frame_dev), 1)
    row = iota((rows, 1), 0)
    inner = jnp.where((lane > 0) & (lane < frame_dev - 1), usable, 0.0)
    number = (rows - 2) * jnp.sum(inner, axis=1, keepdims=True)
    inner = inner * ((row > 0) & (row < rows - 1)).astype(F32)
    centre = jnp.sum(jnp.sum(x, axis=0, keepdims=True), axis=1, keepdims=True)
    centre = centre / (rows * jnp.maximum(jnp.sum(usable, axis=1, keepdims=True), 1.0))
    centre = lax.reduce_precision(centre, 8, 7)
    shifted = [pltpu.roll(x, 1, 1) * behind, x, pltpu.roll(x, frame_dev - 1, 1) * ahead]
    taps = [pltpu.roll(v, (1 - i) % rows, 0) if i != 1 else v for i in range(3) for v in shifted]
    features = feature_rows(centre, (taps, inner))
    lane = iota((1, 128), 1)
    features = jnp.where(lane == 90, centre, jnp.where(lane == 91, number, features))
    pick = iota((8, frame_dev), 0)
    column = jnp.where(pick < 4, pick, frame_dev - 8 + pick)
    strip = dot((iota((8, frame_dev), 1) == column).astype(BF16), x.astype(BF16), ((1,), (1,)))
    lane = iota((8, 128), 1)
    repeat = (iota((rows, 128), 1) % rows == iota((rows, 128), 0)).astype(BF16)
    strip = jnp.where(lane // rows == iota((8, 128), 0), dot(strip.astype(BF16), repeat), 0.0)
    strip = jnp.sum(strip, axis=0, keepdims=True)

    def put(n, value):
        rows_out[pl.ds(n, devices, stride=FIRST), :] = jnp.broadcast_to(value, (devices, 128))

    near = jnp.concatenate([x[0:4], x[rows - 4 :]], axis=0)
    near = jnp.concatenate([near[:, :128], near[:, 128:]], axis=0)
    for d in range(devices):
        rows_out[FIRST * d : FIRST * d + 16, :] = near
    put(COLUMNS, strip)
    copies[2].wait()
    _, chan, many, half = own.shape
    share = share_of(devices, chan)
    holders = chan // share
    g = own[0].astype(F32)
    edges[0:chan] = g[:, 0, :]
    edges[chan:] = g[:, many - 1, :]

    def spread_out(v):
        if holders < devices:
            v = jnp.concatenate([v, jnp.zeros((devices - holders, 128), F32)], axis=0)
        return v

    for n in range(share):
        put(EDGES + n, spread_out(edges[n * holders : (n + 1) * holders, :]))
        put(EDGES + share + n, spread_out(edges[chan + n * holders : chan + (n + 1) * holders, :]))
    for n in range(2 * share, COLUMNS - EDGES):
        put(EDGES + n, jnp.zeros((1, 128), F32))
    end = iota((8, half), 0)
    at = iota((8, half), 1)
    ends = ((end == 0) & (at == 0)) | ((end == 1) & (at == half - 1))
    columns = dot(ends.astype(BF16), g.reshape(chan * many, half).astype(BF16), ((1,), (1,)))
    group = 128 // many
    source = iota((128, 128), 0)
    lane = iota((group, 128), 1)
    mine = lane // many == iota((group, 128), 0)
    parts = three_parts(features)
    for n in range(2):
        side = jnp.zeros((holders, 128), F32)
        for m in range(share):
            move = (iota((128, 128), 1) == SIDE + many * m + source % many).astype(BF16)
            first = m * holders * many // 128
            block = [columns[n : n + 1, 128 * q : 128 * (q + 1)] for q in range(first, first + holders * many // 128)]
            block = jnp.concatenate([jnp.where(mine, v, 0.0) for v in block], axis=0)
            side = side + dot(block.astype(BF16), move)
        put(SUMS + n, spread_out(side) + parts[n])
    put(SUMS + 2, parts[2])
    out[...] = rows_out[...].reshape(out.shape).astype(BF16)


def weights(own, bounds_hbm, k2_hbm, k1_hbm, gain_one_hbm, bias_one_hbm, gain_two_hbm, bias_two_hbm,
            wf, wb, w1, ws_hbm, pairs, singles, k1t, params, all_masks, edge_masks, twice, own_rows,
            k2, k1, vectors, bounds, ws, temp, sems):
    loads = start_all(
        (bounds_hbm, bounds),
        (k2_hbm, k2),
        (k1_hbm, k1),
        (gain_one_hbm, vectors.at[0]),
        (bias_one_hbm, vectors.at[1]),
        (gain_two_hbm, vectors.at[2]),
        (bias_two_hbm, vectors.at[3]),
        sems=sems,
    )
    _, many, count, half = own.shape
    temp[...] = own[0].astype(F32).reshape(many * count, half)
    for r in range(count):
        own_rows[r * many : (r + 1) * many] = temp[pl.ds(r, many, stride=count), :].astype(BF16)
    wait_all(loads)
    chan = k2.shape[1]
    span = wf.shape[1]
    taps = [k2[t].astype(F32) for t in range(9)]
    rest = jnp.zeros((chan, span - 9 * chan), F32)
    forward = jnp.concatenate(taps + [rest], axis=1)
    backward = jnp.concatenate([taps[8 - t].T for t in range(9)] + [rest], axis=1)
    for r in range(wb.shape[0] // chan):
        at = slice(r * chan, (r + 1) * chan)
        wb[at] = (pltpu.roll(backward, 3 * chan * r, 1) if r else backward).astype(BF16)
    full = jnp.concatenate([k1[n].astype(F32) for n in range(3)] + [jnp.zeros((7, chan), F32)], axis=0)
    low = [
        jnp.concatenate([full[3 * (2 - a) + 2 - b : 3 * (2 - a) + 3 - b] for a in range(3)], axis=1)
        for b in range(3)
    ]
    rest = jnp.zeros((1, ws.shape[1] - 3 * chan), F32)
    for b in range(3):
        base = jnp.concatenate([low[b], rest], axis=1)
        many = ws.shape[0] // 3
        rolled = [pltpu.roll(base, chan * m, 1) if m else base for m in range(many)]
        ws[many * b : many * (b + 1)] = jnp.concatenate(rolled, axis=0).astype(BF16)
    store_ws = pltpu.make_async_copy(ws, ws_hbm, sems.at[7])
    store_ws.start()
    count, frame_dev = all_masks.shape[0] // 3, all_masks.shape[1]
    frames = iota((count, frame_dev), 0) * frame_dev + iota((count, frame_dev), 1)
    for n, mask in enumerate(frame_masks(bounds, frames)):
        all_masks[n * count : (n + 1) * count] = mask
    q = iota(edge_masks.shape, 0)
    lane = iota(edge_masks.shape, 1)
    k = q % 8
    frames = (q // 8) * frame_dev + jnp.where(k < 4, k, k + frame_dev - 8)
    living, behind, ahead = frame_masks(bounds, frames)
    living = jnp.where((k == 0) | (k == 7), living, 0.0)
    edge_masks[...] = jnp.where(lane == 0, living, jnp.where(lane == 1, behind, jnp.where(lane == 2, ahead, 0.0)))
    params[...] = jnp.concatenate(
        [vectors[n] for n in range(4)] + [jnp.zeros((4, chan), F32)], axis=0
    )
    tap = iota((16, 128), 0)
    lane = iota((16, 128), 1)
    i = (tap * 11) >> 5
    ninth = (lane * 57) >> 9
    to_band = (lane == BAND * (tap - 3 * i) + i) & (tap < 9)
    to_left = (ninth == tap) & (tap < 9)
    to_right = (lane - 9 * ninth == tap) & (lane < 81)
    to_single = (lane == 81 + tap) & (tap < 9)
    source = iota((128, 128), 0) - 81
    lane = iota((128, 128), 1)
    ninth = (lane * 57) >> 9
    inside = (source >= 0) & (source < 9) & (lane < 81)
    twice[...] = jnp.where(inside, (source == ninth).astype(F32) + (source == lane - 9 * ninth).astype(F32), 0.0)
    for r in range(wf.shape[0] // chan):
        at = slice(r * chan, (r + 1) * chan)
        wf[at] = (pltpu.roll(forward, 3 * chan * r, 1) if r else forward).astype(BF16)
    k1t[...] = full
    k = full.astype(BF16)
    lanes = [dot(k, select.astype(BF16), ((0,), (0,))) for select in (to_band, to_left, to_right, to_single)]
    pairs[...] = lanes[1] * lanes[2]
    singles[...] = lanes[3]
    for m in range(w1.shape[0] // chan):
        w1[m * chan : (m + 1) * chan] = (pltpu.roll(lanes[0], m, 1) if m else lanes[0]).astype(BF16)
    store_ws.wait()


def feature_rows(centre, *parts):
    def folded(v):
        return jnp.sum(halves(v), axis=0, keepdims=True)

    rows = [jnp.zeros((1, 128), F32)] * 96
    for taps, weight in parts:
        z = [tap - centre for tap in taps]
        for s in range(9):
            left = z[s] * weight
            rows[81 + s] = rows[81 + s] + folded(left)
            for t in range(s, 9):
                rows[9 * s + t] = rows[9 * t + s] = rows[9 * s + t] + folded(left * z[t])
    return to_lanes(jnp.sum(jnp.concatenate(rows, axis=0), axis=1, keepdims=True))


def summed_blocks(ref, devices, by=1):
    block = ref.shape[0] // devices
    period = max(8 // math.gcd(block, 8), by)
    step = period * block
    total = ref[0:step, :]
    for at in range(step, ref.shape[0], step):
        total = total + ref[at : at + step, :]
    results = []
    for first in range(by):
        result = total[first * block : (first + 1) * block]
        for n in range(first + by, period, by):
            result = result + total[n * block : (n + 1) * block]
        results.append(result)
    return results if by > 1 else results[0]


def moved_rows(v, step):
    if step == 0:
        return v
    count = v.shape[0]
    if abs(step) >= count:
        return jnp.zeros_like(v)
    zero = jnp.zeros((abs(step), v.shape[1]), v.dtype)
    if step > 0:
        return jnp.concatenate([zero, v[: count - step]], axis=0)
    return jnp.concatenate([v[-step:], zero], axis=0)


def silu_halves(h):
    t = jnp.tanh(h)
    one = 1.0 + t
    return h * one, one * (1.0 + h * (1.0 - t))


def act_row(act, r, low, low_masks):
    low = low * low_masks[0]
    chan = low.shape[0]
    for n, v in enumerate((low,) + shifted_frames(low, *low_masks[1:])):
        at = (3 * r + (1, 0, 2)[n]) * chan
        act[at : at + chan, :] = v


def forward_one(recv, spec, pairs, singles, twice, w1, wf, params, masks, all_masks, edge_masks,
                pre_two, payload, act, x3, stats, features_out, pre_one, got, strips, halo, rows_out):
    devices = recv.shape[0]
    n_mel, count = lax.axis_size("mel"), lax.axis_size("tm")
    rows = MEL_ROWS
    mels = n_mel * rows
    wide = masks.shape[1]
    frame_dev = wide - RIM
    chan = params.shape[1]
    me_m, me_t = lax.axis_index("mel"), lax.axis_index("tm")
    usable, behind, ahead = (masks[n : n + 1] for n in range(3))
    total = masks[3:4, 0:1]
    got[...] = recv[...].astype(F32).reshape(devices * FIRST, 128)

    def every(n):
        return got[pl.ds(n, devices, stride=FIRST), :]

    lane = iota((count, 128), 1)
    bands = [got[pl.ds(FIRST * k * count + COLUMNS, count, stride=FIRST), :] for k in range(n_mel)]
    for c in range(8):
        column = jnp.zeros((count, 128), F32)
        for k, band in enumerate(bands):
            part = jnp.where(lane // rows == c, band, 0.0)
            column = column + (pltpu.roll(part, rows * (k - c) % 128, 1) if k != c else part)
        strips[pl.ds(c, count, stride=8), :] = column
    at = pl.multiple_of(FIRST * (jnp.maximum(me_m - 1, 0) * count + me_t), 8)
    above = got[pl.ds(at, 16), :] * (me_m > 0).astype(F32)
    at = pl.multiple_of(FIRST * (jnp.minimum(me_m + 1, n_mel - 1) * count + me_t), 8)
    below = got[pl.ds(at, 16), :] * (me_m < n_mel - 1).astype(F32)
    above = jnp.concatenate([above[4:8], above[12:16]], axis=1)
    below = jnp.concatenate([below[0:4], below[8:12]], axis=1)
    own = spec[0].astype(F32) * usable[:, :frame_dev]
    at = pl.multiple_of(8 * jnp.minimum(me_t + 1, count - 1), 8)
    after = strips[pl.ds(at, 8), :][:, :mels] * (me_t + 1 < count).astype(F32)
    at = pl.multiple_of(8 * jnp.maximum(me_t - 1, 0), 8)
    before = strips[pl.ds(at, 8), :][:, :mels] * (me_t > 0).astype(F32)
    sides = jnp.concatenate([after[0:4], before[4:8], jnp.zeros((8, mels), F32)], axis=0).astype(BF16)
    side = iota((16, RIM), 0)
    place = iota((16, RIM), 1) == jnp.where(side < 4, side, jnp.where(side < 8, side + RIM - 8, -1))
    halo[0:8] = jnp.zeros((8, RIM), F32)
    halo[mels : mels + 8] = jnp.zeros((8, RIM), F32)
    halo[4 : mels + 4] = dot(sides, place.astype(BF16), ((0,), (0,)))
    rim = halo[pl.ds(pl.multiple_of(me_m * rows, 8), BAND), :]
    near = jnp.concatenate([jnp.concatenate([above, own, below], axis=0), rim], axis=1)
    x3[...] = jnp.concatenate(
        [
            pltpu.roll(near, 1, 1) * behind,
            near,
            pltpu.roll(near, wide - 1, 1) * ahead,
            jnp.broadcast_to(usable, (BAND, wide)),
            jnp.zeros((128 - 4 * BAND, wide), F32),
        ],
        axis=0,
    ).astype(BF16)
    pre_one[2 * chan : (rows + 4) * chan] = dot(w1[2 * chan : (rows + 4) * chan, :], x3[...])
    lane = iota((1, 128), 1)
    parts = jnp.where(lane < 92, every(SUMS) + every(SUMS + 1) + every(SUMS + 2), 0.0)
    centres, numbers = parts[:, 90:91], parts[:, 91:92]
    centre = jnp.sum(centres * numbers, axis=0, keepdims=True)
    centre = centre / jnp.maximum(jnp.sum(numbers, axis=0, keepdims=True), 1.0)
    delta = centres - centre
    features = jnp.sum(parts + delta * numbers * jnp.where(lane < 81, delta, 1.0), axis=0, keepdims=True)
    moved = jnp.sum(delta * parts, axis=0, keepdims=True)
    def edge_row(k, n):
        first = FIRST * k * count + n
        return jnp.concatenate(
            [got[pl.ds(first, count, stride=FIRST), :], got[pl.ds(first + 8, count, stride=FIRST), :]], axis=1
        )

    edge_rows = [[edge_row(k, n) for n in (0, 1, 6, 7)] for k in range(n_mel)]
    zero = jnp.zeros((count, frame_dev), F32)
    rows_of = [[], [], []]
    for k, (top, second, fore, bottom) in enumerate(edge_rows):
        for n, v in enumerate((edge_rows[k - 1][3] if k else zero, top, second)):
            rows_of[n].append(v)
        for n, v in enumerate((fore, bottom, edge_rows[k + 1][0] if k + 1 < n_mel else zero)):
            rows_of[n].append(v)
    f_usable, f_behind, f_ahead = (all_masks[n * count : (n + 1) * count, :] for n in range(3))
    lane = iota((count, frame_dev), 1)

    def frame_before(v):
        v = pltpu.roll(v, 1, 1)
        return jnp.where(lane == 0, pltpu.roll(v, 1, 0), v) * f_behind

    def frame_after(v):
        v = pltpu.roll(v, frame_dev - 1, 1)
        return jnp.where(lane == frame_dev - 1, pltpu.roll(v, count - 1, 0), v) * f_ahead

    taps = []
    for group in rows_of:
        for move in (frame_before, lambda v: v, frame_after):
            taps.append(jnp.concatenate([move(v) for v in group], axis=1))
    f_usable = jnp.concatenate([f_usable] * (2 * n_mel), axis=1)
    borders = (taps, f_usable)
    edge = strips[...]
    q_usable, q_behind, q_ahead = (edge_masks[:, n : n + 1] for n in range(3))
    lane = iota((count * 8, 128), 1)
    inside = (lane < mels) & (lane % rows != 0) & (lane % rows != rows - 1)
    shifted = [
        pltpu.roll(edge, 1, 0) * q_behind,
        edge,
        pltpu.roll(edge, count * 8 - 1, 0) * q_ahead,
    ]
    taps = [pltpu.roll(v, (1 - i) % 128, 1) if i != 1 else v for i in range(3) for v in shifted]
    features = features + feature_rows(centre, borders, (taps, jnp.where(inside, q_usable, 0.0)))
    features = jnp.where(iota((1, 128), 1) < 90, features, 0.0)
    near_mean = jnp.sum(singles[...] * features, axis=1, keepdims=True) / total
    around = jnp.sum(singles[...], axis=1, keepdims=True)
    square = jnp.sum(pairs[...] * features, axis=1, keepdims=True)
    square = (square + 2.0 * around * jnp.sum(singles[...] * moved, axis=1, keepdims=True)) / total
    inv = lax.rsqrt(square - near_mean * near_mean + 1e-05)
    mean = near_mean + centre * around
    lane = iota((chan, 128), 1)
    stats[0:chan] = jnp.where(lane == 0, mean, jnp.where(lane == 1, inv, 0.0))
    stats[chan : chan + 8] = jnp.broadcast_to(to_lanes(near_mean), (8, 128))
    stats[chan + 8 : chan + 16] = jnp.broadcast_to(to_lanes(inv), (8, 128))
    scale = 0.5 * to_column(params[0:1], chan) * inv
    shift = 0.5 * to_column(params[1:2], chan) - mean * scale
    stats[chan + 16 :] = jnp.where(lane == 0, scale, jnp.where(lane == 1, shift, 0.0))
    scale = jnp.broadcast_to(scale, (chan, wide))
    shift = jnp.broadcast_to(shift, (chan, wide))
    block, taps = wf.shape
    first = jnp.zeros((chan, 128), F32)
    second = jnp.zeros((chan, 128), F32)
    own_mask = usable[:, :frame_dev]
    low_masks = [m.astype(BF16) for m in (usable, behind, ahead)]
    for r in range(2, rows + 4):
        value, _ = silu_halves(pre_one[r * chan : (r + 1) * chan, :] * scale + shift)
        if not 0 <= r - 3 < rows:
            value = value * row_valid(r - 3, rows)
        act_row(act, r, value.astype(BF16), low_masks)
        if r < 5 or r % 2 == 0:
            continue
        g = (r - 3) // 2
        result = dot(wf[...], act[g * 3 * block : g * 3 * block + taps, :frame_dev])
        at = (g - 1) * block
        pre_two[at : at + block, :frame_dev] = result
        if g % 2 == 0:
            beside = [act[n * 3 * block : n * 3 * block + taps, frame_dev:] for n in (g - 1, g)]
            beside = dot(wf[...], jnp.concatenate(beside, axis=1))
            for n in range(2):
                pre_two[at + (n - 1) * block : at + n * block, frame_dev:] = beside[:, n * RIM : (n + 1) * RIM]
        for q in range(2):
            p = result[q * chan : (q + 1) * chan]
            masked = p * own_mask
            first = first + halves(masked)
            second = second + halves(masked * p)
    moved = dot(jnp.broadcast_to(moved, (8, 128)), twice[...], precision=EXACT)[0:1]
    features_out[...] = jnp.concatenate(
        [features + moved, jnp.broadcast_to(centre, (1, 128)), jnp.zeros((6, 128), F32)], axis=0
    )
    share = share_of(devices, chan)

    def put(n, value):
        rows_out[pl.ds(n, devices, stride=SECOND), :] = jnp.broadcast_to(value, (devices, 128))

    for n in range(share):
        put(3 + n, moved_rows(every(EDGES + share + n), count))
        put(3 + share + n, moved_rows(every(EDGES + n), -count))
    for n in [0, 1, 2] + list(range(3 + 2 * share, SECOND - 1)):
        put(n, jnp.zeros((1, 128), F32))
    lane = iota((devices, 128), 1)
    tm = iota((devices, 128), 0) % count
    lefts = jnp.where(lane >= SIDE, every(SUMS), 0.0)
    rights = jnp.where(lane >= SIDE, every(SUMS + 1), 0.0)
    beside = jnp.zeros((devices, 128), F32)
    for n, step in enumerate((0, count, -count)):
        one = jnp.where(tm > 0, moved_rows(rights, step + 1), 0.0)
        two = jnp.where(tm < count - 1, moved_rows(lefts, step - 1), 0.0)
        beside = beside + pltpu.roll(one, (32 * n - SIDE) % 128, 1) + pltpu.roll(two, (32 * n + 16 - SIDE) % 128, 1)
    put(SECOND - 1, beside)
    first = jnp.sum(first, axis=1, keepdims=True)
    second = jnp.sum(second, axis=1, keepdims=True)
    parts = list(three_parts(to_lanes(first) + to_lanes(second, chan)))
    parts = jnp.concatenate(parts + [jnp.zeros((SECOND - 3, 128), F32)], axis=0)
    for d in range(devices):
        payload[d] = (rows_out[SECOND * d : SECOND * (d + 1), :] + parts).astype(BF16)


def spreading(half):
    lane = iota((half, 2 * half), 1)
    return jnp.where(lane >> 1 == iota((half, 2 * half), 0), 0.25, 0.0).astype(BF16)


def half_share(devices, taps):
    return -(-taps // 2 // devices)


def backward_scaled(recv, pre_two, act, own_rows, params, masks,
                    grad, kept_half, sent_half, totals, stats, up, right, got, halved):
    devices = recv.shape[0]
    got[...] = recv[:, 0:SECOND, :].astype(F32).reshape(devices * SECOND, 128)
    chan = params.shape[1]
    half = own_rows.shape[1]
    frame_dev = 2 * half
    rows = MEL_ROWS
    up[...] = dot(own_rows[...], spreading(half))
    usable = masks[0:1, :frame_dev]
    total = masks[3:4, 0:1]
    sums = [got[pl.ds(n, devices, stride=SECOND), :] for n in range(3)]
    sums = jnp.sum(sums[0] + sums[1] + sums[2], axis=0, keepdims=True)
    mean = to_column(sums, chan) / total
    inv = lax.rsqrt(to_column(sums, chan, chan) / total - mean * mean + 1e-05)
    scale = 0.5 * to_column(params[2:3], chan) * inv
    shift = 0.5 * to_column(params[3:4], chan) - mean * scale
    lane = iota((chan, 128), 1)
    columns = jnp.zeros((chan, 128), F32)
    for n, column in enumerate((mean, inv, scale, shift)):
        columns = jnp.where(lane == n, column, columns)
    stats[0:chan] = columns
    stats[chan : chan + 8] = jnp.broadcast_to(to_lanes(inv), (8, 128))
    mean, inv, scale, shift = (jnp.broadcast_to(v, (chan, frame_dev)) for v in (mean, inv, scale, shift))
    first = jnp.zeros((chan, 128), F32)
    second = jnp.zeros((chan, 128), F32)
    mask = 0.5 * usable
    right[3 * chan :] = jnp.ones((16, rows * frame_dev), BF16)
    table = jnp.zeros((9 * chan, 3 * chan + 16), F32)
    for m in range(rows):
        at = slice(m * chan, (m + 1) * chan)
        pre = pre_two[at, :frame_dev]
        _, slope = silu_halves(pre * scale + shift)
        g = up[m // 2 * chan : (m // 2 + 1) * chan, :] * slope * mask
        grad[at, :] = g
        normed = (pre - mean) * inv
        first = first + halves(g * normed)
        second = second + halves(g)
        lanes = slice(m * frame_dev, (m + 1) * frame_dev)
        right[0:chan, lanes] = g.astype(BF16)
        right[chan : 2 * chan, lanes] = normed.astype(BF16)
        right[2 * chan : 3 * chan, lanes] = (g - right[0:chan, lanes].astype(F32)).astype(BF16)
        if m in (5, 11, rows - 1):
            start = m - m % 6
            left = [act[(n + 2) * 3 * chan : (n + 5) * 3 * chan, :frame_dev] for n in range(start, m + 1)]
            lanes = slice(start * frame_dev, (m + 1) * frame_dev)
            table = table + dot(jnp.concatenate(left, axis=1), right[:, lanes], ((1,), (1,)))
    first = jnp.sum(first, axis=1, keepdims=True)
    second = jnp.sum(second, axis=1, keepdims=True)
    totals[...] = jnp.broadcast_to(to_lanes(first) + to_lanes(second, chan), (8, 128))
    rest = jnp.concatenate([table[:, 2 * chan :], jnp.zeros((9 * chan, chan - 16), F32)], axis=1)
    both = table[:, : 2 * chan] + jnp.where(iota(rest.shape, 1) < chan, rest, 0.0)
    single = rest[:, chan : chan + 1]
    taps = 9 * chan // 2
    lane = iota((devices, 128), 1)
    for h in range(2):
        halved[h, 0:taps] = both[h * taps : (h + 1) * taps]
        constants = jnp.zeros((devices, 128), F32)
        for k in range(half_share(devices, 9 * chan)):
            at = h * taps + k * devices
            ones = single[at : min(at + devices, (h + 1) * taps)]
            if ones.shape[0] < devices:
                ones = jnp.concatenate([ones, jnp.zeros((devices - ones.shape[0], 1), F32)], axis=0)
            constants = jnp.where(lane == k, ones, constants)
        halved[h, taps:] = constants
    core = lax.axis_index("tm") % 2
    kept_half[...] = halved[core]
    sent_half[...] = halved[1 - core]


def around(recv, pre_two, act, w1, wf, x3, stats_one, masks, stats, pre_ring, ring, rim, pairs,
           sides, up, got, beyond, more):
    devices = recv.shape[0]
    got[...] = recv[:, 0:SECOND, :].astype(F32).reshape(devices * SECOND, 128)
    rows = MEL_ROWS
    many = rows // 2
    wide = pre_two.shape[1]
    frame_dev = wide - RIM
    chan = pre_two.shape[0] // rows
    usable = masks[0:1]
    low_masks = [masks[n : n + 1].astype(BF16) for n in range(3)]
    scale = jnp.broadcast_to(stats_one[chan + 16 :, 0:1], (chan, wide))
    shift = jnp.broadcast_to(stats_one[chan + 16 :, 1:2], (chan, wide))
    for h, start in enumerate((0, rows + 4)):
        pre_one = dot(w1[start * chan : (start + 2) * chan, :], x3[...])
        for n in range(2):
            value, _ = silu_halves(pre_one[n * chan : (n + 1) * chan] * scale + shift)
            value = value * row_valid(start + n - 3, rows)
            act_row(more, 2 * h + n, value.astype(BF16), low_masks)
    line = 3 * chan
    above = jnp.concatenate([more[0 : 2 * line, :], act[2 * line : 4 * line, :]], axis=0)
    below = jnp.concatenate([act[(rows + 2) * line : (rows + 4) * line, :], more[2 * line :, :]], axis=0)
    pre_ring[0 : 2 * chan] = dot(wf[...], above)
    pre_ring[2 * chan :] = dot(wf[...], below)
    share = share_of(devices, chan)
    holders = chan // share

    def every(n):
        return got[pl.ds(n, devices, stride=SECOND), :]

    beside = every(SECOND - 1)[:holders]
    lane = iota((holders, RIM), 1)
    for n in range(share):
        first = n * holders
        beyond[first : first + holders, :] = every(3 + n)[:holders]
        beyond[chan + first : chan + first + holders, :] = every(3 + share + n)[:holders]
        for r in range(many + 2):
            at = many * n + (r if r < many else 32 + many - 1 if r == many else 64)
            left, right_of = beside[:, at : at + 1], beside[:, at + 16 : at + 17]
            side = jnp.where(lane >= RIM - 2, 0.25 * left, jnp.where(lane < 2, 0.25 * right_of, 0.0))
            sides[r * chan + first : r * chan + first + holders, :] = side
    up[...] = dot(beyond[...].astype(BF16), spreading(frame_dev // 2))
    scale = jnp.broadcast_to(stats[0:chan, 2:3], (chan, wide))
    shift = jnp.broadcast_to(stats[0:chan, 3:4], (chan, wide))
    for n, m in enumerate((-2, -1, rows, rows + 1)):
        below = n // 2
        upstream = jnp.concatenate(
            [
                up[below * chan : (below + 1) * chan, :],
                sides[(many + below) * chan : (many + below + 1) * chan, :],
            ],
            axis=1,
        )
        _, slope = silu_halves(pre_ring[n * chan : (n + 1) * chan, :] * scale + shift)
        ring[n * chan : (n + 1) * chan, :] = upstream * slope * (usable * (0.5 * row_valid(m, rows)))
    both = None
    for m in range(rows):
        at = slice(m * chan, (m + 1) * chan)
        _, slope = silu_halves(pre_two[at, frame_dev:] * scale[:, frame_dev:] + shift[:, frame_dev:])
        upstream = sides[m // 2 * chan : (m // 2 + 1) * chan, :]
        rim[m * chan : (m + 1) * chan, :] = upstream * slope * (0.5 * usable[:, frame_dev:])
        value, _ = silu_halves(pre_two[at, :frame_dev] * scale[:, :frame_dev] + shift[:, :frame_dev])
        value = value * usable[:, :frame_dev]
        both = value if m % 2 == 0 else both + value
        if m % 2:
            pairs[m // 2 * chan : (m // 2 + 1) * chan, :] = both


def pack_sums(kept_half, received, totals, after, payload):
    del after
    devices = kept_half.shape[0] - TAPS // 2
    block = payload.shape[0] // devices
    payload[pl.ds(0, devices, stride=block), :] = jnp.broadcast_to(totals[0:1], (devices, 128))
    taps = TAPS // 2
    total = kept_half[...] + received[...]
    for k in range(block - 2):
        cut = total[k * devices : min((k + 1) * devices, taps)]
        if cut.shape[0] < devices:
            cut = jnp.concatenate([cut, jnp.zeros((devices - cut.shape[0], 128), F32)], axis=0)
        payload[pl.ds(1 + k, devices, stride=block), :] = cut
    payload[pl.ds(block - 1, devices, stride=block), :] = total[taps:]


def pool(totals, pairs, out, gain_out, bias_out, temp):
    gain_out[...] = totals[0:1, : gain_out.shape[1]]
    bias_out[...] = totals[0:1, gain_out.shape[1] :]
    chan, rows, half = out.shape[1:]
    to_mean = jnp.where(iota((2 * half, half), 0) >> 1 == iota((2 * half, half), 1), 0.25, 0.0)
    pooled = dot(pairs[...], to_mean, precision=EXACT)
    for r in range(rows):
        temp[pl.ds(r, chan, stride=rows), :] = pooled[r * chan : (r + 1) * chan]
    out[0] = temp[...].reshape(chan, rows, half).astype(BF16)


def backward(recv, pre_two, pre_ring, grad, ring, rim, stats_two, w1, x3, stats, params, masks, wb,
             out, own_low, payload, totals, g3, pre_one, g1):
    chan = params.shape[1]
    rows = MEL_ROWS
    wide = pre_two.shape[1]
    frame_dev = wide - RIM
    usable = masks[0:1]
    behind, ahead = (masks[n : n + 1].astype(BF16) for n in (1, 2))
    total = masks[3:4, 0:1]
    devices = payload.shape[0] // 14
    pre_one[...] = dot(w1[3 * chan : (rows + 3) * chan], x3[:, :frame_dev])

    even, odd = summed_blocks(recv, devices, 2)
    sums = even[0:1] + odd[0:1]
    gain_sum, bias_sum = sums[:, :chan], sums[:, chan:]
    totals[...] = jnp.broadcast_to(sums, (8, 128))
    mean, inv = stats_two[0:chan, 0:1], stats_two[0:chan, 1:2]
    factor = to_column(params[2:3], chan) * inv
    gain_part = factor * (to_column(sums, chan) / total * inv)
    bias_part = factor * (to_column(sums, chan, chan) / total) - mean * gain_part
    gain_part = jnp.broadcast_to(gain_part, (chan, wide))
    bias_part = jnp.broadcast_to(bias_part, (chan, wide))
    factor = jnp.broadcast_to(factor, (chan, wide))
    scale = jnp.broadcast_to(stats[chan + 16 :, 0:1], (chan, frame_dev))
    shift = jnp.broadcast_to(stats[chan + 16 :, 1:2], (chan, frame_dev))
    factor_one = jnp.broadcast_to(to_column(params[0:1], chan) * stats[0:chan, 1:2], (chan, frame_dev))
    own_mask = 0.5 * usable[:, :frame_dev]
    count = rows + 4
    share = even.shape[0] - 2
    mine = jnp.concatenate([even[1 : share + 1], odd[1 : share + 1]], axis=0)
    single = jnp.concatenate([to_column(v[share + 1 :], share) for v in (even, odd)], axis=0)
    factor_l = params[2:3] * stats_two[chan : chan + 1, :chan]
    mine = mine[:, :chan] - (bias_sum * single + gain_sum * mine[:, chan:]) / total
    mine = factor_l * mine
    mine = jnp.concatenate([mine[:share], mine[share:]], axis=1)
    if share < 9:
        mine = jnp.concatenate([mine, jnp.zeros((9 - share, 128), F32)], axis=0)
    table = jnp.zeros((chan, 128), F32)

    def tap_sums(m):
        part = g1[m * chan : (m + 4) * chan, :]
        high = lax.reduce_precision(part, 8, 7)
        low = (part - high).astype(BF16)
        taps_in = x3[:, :frame_dev]
        products = dot(high.astype(BF16), taps_in, ((1,), (1,))) + dot(low, taps_in, ((1,), (1,)))
        moved = [pltpu.roll(products[k * chan : (k + 1) * chan], 128 - (m + k + 3), 1) for k in range(4)]
        return (moved[0] + moved[1]) + (moved[2] + moved[3])

    for q in range(count):
        at = slice(q * chan, (q + 1) * chan)
        mask = usable if 0 <= q - 2 < rows else usable * row_valid(q - 2, rows)
        if 2 <= q < rows + 2:
            own = slice((q - 2) * chan, (q - 1) * chan)
            pre, scaled = pre_two[own, :], jnp.concatenate([grad[own, :], rim[own, :]], axis=1)
        else:
            n = q if q < 2 else q - rows
            pre, scaled = pre_ring[n * chan : (n + 1) * chan, :], ring[n * chan : (n + 1) * chan, :]
        low = (factor * scaled - (bias_part + pre * gain_part) * mask).astype(BF16)
        out[at, :] = low
        if not 1 <= q < count - 1:
            continue
        base = (q - 1) * 3 * chan
        for n, v in enumerate((low,) + shifted_frames(low, behind, ahead)):
            spot = base + (1, 0, 2)[n] * chan
            g3[spot : spot + chan, :] = v[:, :frame_dev]
        start = q - 4
        if start < 0 or start % 2:
            continue
        result = dot(wb[...], g3[start * 3 * chan : (start + 4) * 3 * chan, :])
        for n in range(2):
            m = start + n
            at = slice(m * chan, (m + 1) * chan)
            _, slope = silu_halves(pre_one[at, :] * scale + shift)
            value = result[n * chan : (n + 1) * chan] * slope * own_mask
            own_low[at, :] = (value * factor_one).astype(BF16)
            g1[at, :] = value
        if start % 4 == 2 and start > 2:
            table = table + tap_sums(start - 6)
    table = table + tap_sums(rows - 4)
    table = table.T
    places = [BAND * j + i for i in range(3) for j in range(3)] + [3 * BAND]
    rows10 = jnp.concatenate([table[n : n + 1] for n in places], axis=0)
    sums = jnp.concatenate([rows10[0:5], rows10[5:10]], axis=1)
    block = jnp.concatenate([sums, mine], axis=0)
    block = jnp.concatenate([block] * 4, axis=0)
    for d in range(0, devices, 4):
        payload[14 * d : 14 * (d + 4), :] = block


def transposed(grad, own_low, w1, wb, x3, stats, features, k1t, params, masks, ws_hbm,
               first, ws, normed_taps, low, g3, rim, sem):
    load = pltpu.make_async_copy(ws_hbm, ws, sem)
    load.start()
    rows = MEL_ROWS
    chan = own_low.shape[0] // rows
    wide = grad.shape[1]
    frame_dev = wide - RIM
    count = grad.shape[0] // chan
    usable = masks[0:1]
    behind, ahead = (masks[n : n + 1].astype(BF16) for n in (1, 2))
    scale = jnp.broadcast_to(stats[chan + 16 :, 0:1], (chan, wide))
    shift = jnp.broadcast_to(stats[chan + 16 :, 1:2], (chan, wide))
    factor = jnp.broadcast_to(to_column(params[0:1], chan) * stats[0:chan, 1:2], (chan, wide))
    edge = (0, 1, 2, 3, count - 4, count - 3, count - 2, count - 1)
    for q in range(count):
        value = grad[q * chan : (q + 1) * chan, :]
        for n, v in enumerate((value,) + shifted_frames(value, behind, ahead)):
            spot = (3 * q + (1, 0, 2)[n]) * chan
            rim[spot : spot + chan, :] = v[:, frame_dev:]
            if q in edge:
                spot = (3 * edge.index(q) + (1, 0, 2)[n]) * chan
                g3[spot : spot + chan, :] = v[:, :frame_dev]
    low[chan : (rows + 1) * chan, :frame_dev] = own_low[...]

    def put(m, lanes, result, pre_one):
        at = slice((m + 1) * chan, (m + 2) * chan)
        _, slope = silu_halves(pre_one * scale[:, lanes] + shift[:, lanes])
        mask = usable[:, lanes] * (0.5 * row_valid(m, rows))
        low[at, lanes] = (result * slope * mask * factor[:, lanes]).astype(BF16)

    pre_one = dot(w1[2 * chan : (rows + 4) * chan, :], x3[:, frame_dev:])
    beside = slice(frame_dev, wide)
    for start in range(0, rows + 2, 2):
        result = dot(wb[...], rim[start * 3 * chan : (start + 4) * 3 * chan, :])
        for n in range(2):
            at = slice((start + n) * chan, (start + n + 1) * chan)
            put(start + n - 1, beside, result[n * chan : (n + 1) * chan], pre_one[at])
    own = slice(0, frame_dev)
    result = dot(wb[...], g3[: 4 * 3 * chan, :])
    put(-1, own, result[:chan], dot(w1[2 * chan : 3 * chan, :], x3[:, :frame_dev]))
    result = dot(wb[...], g3[4 * 3 * chan :, :])
    put(rows, own, result[chan:], dot(w1[(rows + 3) * chan : (rows + 4) * chan, :], x3[:, :frame_dev]))
    row = features[0:1, :]
    lane = iota((1, 128), 1)
    gram = jnp.concatenate(
        [jnp.where(lane < 9, pltpu.roll(row, 128 - 9 * t, 1) if t else row, 0.0) for t in range(9)]
        + [jnp.zeros((7, 128), F32)],
        axis=0,
    )
    single = to_column(row, 16, 81)[0:9]
    k_rows = jnp.concatenate([k1t[...], jnp.zeros((112, chan), F32)], axis=0)
    mean_l, inv_l = stats[chan : chan + 1, :chan], stats[chan + 8 : chan + 9, :chan]
    normed = inv_l * (dot(gram, k_rows, precision=EXACT)[0:9] - single * mean_l)
    normed_taps[0:16] = jnp.concatenate([normed, jnp.zeros((7, chan), F32)], axis=0)
    normed_taps[16:32] = jnp.broadcast_to(to_column(row, 16, 81), (16, chan))
    load.wait()
    first[...] = dot(ws[...], low[...])


def finish(recv, features, stats, k1t, first, ws, w1, x3, normed_taps, params, masks,
           spec_hbm, kernel_one_hbm, kernel_two_hbm, gain_hbm, bias_hbm,
           spec_grad, kernel_one, kernel_two, gain_out, bias_out, sems):
    chan = params.shape[1]
    rows = MEL_ROWS
    wide = x3.shape[1]
    frame_dev = wide - RIM
    usable, behind, ahead = (masks[n : n + 1] for n in range(3))
    total = masks[3:4, 0:1]
    gain = params[0:1]
    count = recv.shape[0] // 14
    share = half_share(count, 9 * chan)
    sums = summed_blocks(recv, count)[0:5]
    ten = jnp.concatenate([sums[:, :chan], sums[:, chan:]], axis=0)
    bias_sum = ten[9:10]
    mean_l, inv_l = stats[chan : chan + 1, :chan], stats[chan + 8 : chan + 9, :chan]
    ten = ten - features[1:2, 0:1] * bias_sum
    k = k1t[0:9]
    gain_sum = inv_l * (jnp.sum(k * ten[0:9], axis=0, keepdims=True) - mean_l * bias_sum)
    gain_out[...] = gain_sum
    bias_out[...] = bias_sum
    factor_l = gain * inv_l
    scale = factor_l * gain_sum / total * inv_l
    scale = jnp.concatenate(
        [scale * row_valid(-1, rows)] + [scale] * rows + [scale * row_valid(rows, rows)], axis=1
    )
    many = 3 * rows

    def in_parts(v, right):
        high = lax.reduce_precision(v, 8, 7)
        v = dot(jnp.concatenate([high, v - high], axis=0).astype(BF16), right)
        return v[:many] + v[many:]

    combined = in_parts(ws[...].astype(F32) * scale, w1[2 * chan : (rows + 4) * chan, :])
    left = [recv[pl.ds(5 + p, count, stride=14), :] for p in range(share)]
    taps = TAPS // 2
    whole = [jnp.concatenate([v[:, h * chan : (h + 1) * chan] for v in left], axis=0)[:taps] for h in range(2)]
    whole = jnp.concatenate(whole, axis=0)
    for t in range(9):
        kernel_two[t] = whole[t * chan : (t + 1) * chan].T
    stores = [pltpu.make_async_copy(kernel_two, kernel_two_hbm, sems.at[4])]
    stores[0].start()
    taken = in_parts(combined, x3[...])
    taps = first[...] - taken
    moved = [taps[rows * b : rows * (b + 1)] for b in range(3)]
    mean_full = mean_l + features[1:2, 0:1] * jnp.sum(k, axis=0, keepdims=True)
    constant = jnp.sum(k * (factor_l * (bias_sum - gain_sum * inv_l * mean_full) / total), axis=1, keepdims=True)
    for a in range(3):
        row = iota((rows, 1), 0) + (a - 1) + lax.axis_index("mel") * rows
        valid = ((row >= 0) & (row < lax.axis_size("mel") * rows)).astype(F32) * usable
        for b in range(3):
            t = 3 * (2 - a) + 2 - b
            moved[b] = moved[b] - constant[t : t + 1] * valid
    result = pltpu.roll(moved[0], 1, 1) * behind + moved[1] + pltpu.roll(moved[2], wide - 1, 1) * ahead
    spec_grad[0] = (result * usable)[:, :frame_dev]
    grad_taps = factor_l * (ten[0:9] - (bias_sum * normed_taps[16:25] + gain_sum * normed_taps[0:9]) / total)
    for i in range(3):
        kernel_one[i] = grad_taps[3 * i : 3 * i + 3]
    outs = ((spec_grad, spec_hbm), (kernel_one, kernel_one_hbm), (gain_out, gain_hbm), (bias_out, bias_hbm))
    wait_all(stores + start_all(*outs, sems=sems))


def run(kernel, outs, scratch, *args, hbm=0, apart=(), flops=10**8, size=4 * 10**6):
    vmem = pl.BlockSpec(memory_space=pltpu.VMEM)
    devices = lax.axis_size("mel") * lax.axis_size("tm")
    specs = []
    args = list(args)
    for n, a in enumerate(args):
        if hbm and n >= len(args) - hbm:
            specs.append(pl.BlockSpec(memory_space=pltpu.HBM))
            args[n] = pltpu.with_memory_space_constraint(a, pltpu.HBM)
        else:
            specs.append(vmem)
            args[n] = pltpu.with_memory_space_constraint(a, pltpu.VMEM)
    return pl.pallas_call(
        kernel,
        out_shape=outs,
        in_specs=specs,
        out_specs=[pl.BlockSpec(memory_space=pltpu.HBM) if n in apart else vmem for n in range(len(outs))],
        scratch_shapes=scratch,
        compiler_params=pltpu.CompilerParams(vmem_limit_bytes=(29 + devices // 32) * 2**20),
        cost_estimate=pl.CostEstimate(flops=flops, bytes_accessed=size, transcendentals=0),
    )(*args)


def shape(dims, dtype=F32):
    return jax.ShapeDtypeStruct(dims, dtype)


def kept(dims, dtype=F32):
    return pltpu.VMEM(dims, dtype)


def far(dims, dtype=F32):
    return pltpu.HBM(dims, dtype)


def exchange(blocks, axes=AXES):
    return lax.all_to_all(blocks, axes, 0, 0, tiled=True)


def exchange_rows(rows, axes=AXES):
    return exchange(rows[:, None, :], axes)[:, 0, :]


def shards(spectrum, clip_bounds, kernel_one, gain_one, bias_one, kernel_two, gain_two, bias_two, pooled_grad):
    _, rows, frame_dev = spectrum.shape
    chan = kernel_two.shape[0]
    n_mel, n_tm = lax.axis_size("mel"), lax.axis_size("tm")
    devices = n_mel * n_tm
    half = frame_dev // 2
    wide = frame_dev + RIM
    mels = n_mel * rows

    packed, own, spec, masks = run(
        pack,
        [
            kept((devices, FIRST, 128), BF16),
            kept(pooled_grad.shape, BF16),
            kept(spectrum.shape, BF16),
            kept((8, wide)),
        ],
        [
            pltpu.SMEM(clip_bounds.shape, jnp.int32),
            pltpu.VMEM((2 * chan, half), F32),
            pltpu.VMEM((devices * FIRST, 128), F32),
            pltpu.SemaphoreType.DMA((3,)),
        ],
        spectrum,
        pooled_grad,
        clip_bounds,
        hbm=3,
    )
    recv = exchange(packed)
    ext = rows + 6
    span = 4 * 3 * chan
    wf, wb, w1, ws, pairs, singles, k1t, params, all_masks, edge_masks, twice, own_rows = run(
        weights,
        [
            kept((2 * chan, span), BF16),
            kept((2 * chan, span), BF16),
            kept((ext * chan, 128), BF16),
            far((rows * 3, (rows + 2) * chan), BF16),
            kept((chan, 128)),
            kept((chan, 128)),
            kept((16, chan)),
            kept((8, chan)),
            kept((3 * n_tm, frame_dev)),
            kept((n_tm * 8, 128)),
            kept((128, 128)),
            kept((chan * rows // 2, half), BF16),
        ],
        [
            pltpu.VMEM((9, chan, chan), BF16),
            pltpu.VMEM((3, 3, chan), BF16),
            pltpu.VMEM((4, 1, chan), F32),
            pltpu.SMEM(clip_bounds.shape, jnp.int32),
            pltpu.VMEM((rows * 3, (rows + 2) * chan), BF16),
            pltpu.VMEM((chan * rows // 2, half), F32),
            pltpu.SemaphoreType.DMA((8,)),
        ],
        own,
        clip_bounds,
        jnp.transpose(kernel_two, (2, 3, 0, 1)).reshape(9, chan, chan),
        jnp.transpose(kernel_one, (1, 2, 0)),
        gain_one[None],
        bias_one[None],
        gain_two[None],
        bias_two[None],
        hbm=7,
        apart=(3,),
    )
    pre_two, payload, act, x3, stats_one, features = run(
        forward_one,
        [
            kept((rows * chan, wide)),
            kept((devices, SECOND, 128), BF16),
            kept((ext * 3 * chan, wide), BF16),
            kept((128, wide), BF16),
            kept((2 * chan + 16, 128)),
            kept((8, 128)),
        ],
        [
            pltpu.VMEM((ext * chan, wide), F32),
            pltpu.VMEM((devices * FIRST, 128), F32),
            pltpu.VMEM((n_tm * 8, 128), F32),
            pltpu.VMEM((mels + 8, RIM), F32),
            pltpu.VMEM((devices * SECOND, 128), F32),
        ],
        recv,
        spec,
        pairs,
        singles,
        twice,
        w1,
        wf,
        params,
        masks,
        all_masks,
        edge_masks,
    )
    recv = exchange(payload)
    grad, kept_half, sent_half, totals, stats_two = run(
        backward_scaled,
        [
            kept((rows * chan, frame_dev)),
            kept((TAPS // 2 + devices, 128)),
            kept((TAPS // 2 + devices, 128)),
            kept((8, 128)),
            kept((chan + 8, 128)),
        ],
        [
            pltpu.VMEM((rows // 2 * chan, frame_dev), F32),
            pltpu.VMEM((3 * chan + 16, rows * frame_dev), BF16),
            pltpu.VMEM((devices * SECOND, 128), F32),
            pltpu.VMEM((2, TAPS // 2 + devices, 128), F32),
        ],
        recv,
        pre_two,
        act,
        own_rows,
        params,
        masks,
    )
    received = lax.ppermute(sent_half, "tm", [(i, i ^ 1) for i in range(n_tm)])
    pre_ring, ring, rim, row_pairs = run(
        around,
        [kept((4 * chan, wide)), kept((4 * chan, wide)), kept((rows * chan, RIM)), kept((rows // 2 * chan, frame_dev))],
        [
            pltpu.VMEM(((rows // 2 + 2) * chan, RIM), F32),
            pltpu.VMEM((2 * chan, frame_dev), F32),
            pltpu.VMEM((devices * SECOND, 128), F32),
            pltpu.VMEM((2 * chan, half), F32),
            pltpu.VMEM((4 * 3 * chan, wide), BF16),
        ],
        recv,
        pre_two,
        act,
        w1,
        wf,
        x3,
        stats_one,
        masks,
        stats_two,
    )
    (payload,) = run(
        pack_sums,
        [kept((devices * (half_share(devices, 9 * chan) + 2), 128))],
        [],
        kept_half,
        received,
        totals,
        rim,
    )
    recv = exchange_rows(payload)
    grad, own_low, payload, totals = run(
        backward,
        [
            kept(((rows + 4) * chan, wide), BF16),
            kept((rows * chan, frame_dev), BF16),
            kept((devices * 14, 128)),
            kept((8, 128)),
        ],
        [
            pltpu.VMEM(((rows + 2) * 3 * chan, frame_dev), BF16),
            pltpu.VMEM((rows * chan, frame_dev), F32),
            pltpu.VMEM((rows * chan, frame_dev), F32),
        ],
        recv,
        pre_two,
        pre_ring,
        grad,
        ring,
        rim,
        stats_two,
        w1,
        x3,
        stats_one,
        params,
        masks,
        wb,
    )
    recv = exchange_rows(payload)
    pooled, gain_two_grad, bias_two_grad = run(
        pool,
        [shape((1, chan, rows // 2, half), BF16), shape((1, chan)), shape((1, chan))],
        [
            pltpu.VMEM((rows // 2 * chan, 128), F32),
        ],
        totals,
        row_pairs,
    )
    first, ws, normed_taps = run(
        transposed,
        [
            kept((rows * 3, wide)),
            kept((rows * 3, (rows + 2) * chan), BF16),
            kept((32, chan)),
        ],
        [
            pltpu.VMEM(((rows + 2) * chan, wide), BF16),
            pltpu.VMEM((8 * 3 * chan, frame_dev), BF16),
            pltpu.VMEM(((rows + 4) * 3 * chan, RIM), BF16),
            pltpu.SemaphoreType.DMA,
        ],
        grad,
        own_low,
        w1,
        wb,
        x3,
        stats_one,
        features,
        k1t,
        params,
        masks,
        ws,
        hbm=1,
    )
    spec_grad, kernel_one_grad, kernel_two_grad, gain_one_grad, bias_one_grad = run(
        finish,
        [
            shape((1, rows, frame_dev)),
            shape((3, 3, chan)),
            shape((9, chan, chan)),
            shape((1, chan)),
            shape((1, chan)),
        ],
        [
            pltpu.VMEM((1, rows, frame_dev), F32),
            pltpu.VMEM((3, 3, chan), F32),
            pltpu.VMEM((9, chan, chan), F32),
            pltpu.VMEM((1, chan), F32),
            pltpu.VMEM((1, chan), F32),
            pltpu.SemaphoreType.DMA((5,)),
        ],
        recv,
        features,
        stats_one,
        k1t,
        first,
        ws,
        w1,
        x3,
        normed_taps,
        params,
        masks,
        apart=range(5),
    )
    kernel_two_grad = jnp.transpose(kernel_two_grad.reshape(3, 3, chan, chan), (2, 3, 0, 1))
    return (
        pooled,
        spec_grad,
        jnp.transpose(kernel_one_grad, (2, 0, 1)),
        gain_one_grad[0],
        bias_one_grad[0],
        kernel_two_grad,
        gain_two_grad[0],
        bias_two_grad[0],
    )


def solution(mesh):
    return jax.shard_map(
        shards,
        mesh=mesh,
        in_specs=(
            P(None, "mel", "tm"),
            P(),
            P(),
            P(),
            P(),
            P(),
            P(),
            P(),
            P(None, None, "mel", "tm"),
        ),
        out_specs=(P(None, None, "mel", "tm"), P(None, "mel", "tm"), P(), P(), P(), P(), P(), P()),
        check_vma=False,
    )
```

```python
import math

import jax
import jax.numpy as jnp
from jax import lax
from jax.experimental import pallas as pl
from jax.experimental.pallas import tpu as pltpu
from jax.sharding import PartitionSpec as P

F32 = jnp.float32
BF16 = jnp.bfloat16
AXES = ("mel", "tm")
EXACT = lax.Precision.HIGHEST
RIM = 128
BAND = 24
MEL_ROWS = 16
FIRST = 16
SUMS, EDGES, COLUMNS = 8, 11, 15
SIDE, FAR = 96, 112
FAR_HOLDERS = 32
TAPS = 576
SECOND = 8


def iota(shape, dim):
    return lax.broadcasted_iota(jnp.int32, shape, dim)


def dot(a, b, over=((1,), (0,)), precision=None):
    return lax.dot_general(a, b, (over, ((), ())), precision=precision, preferred_element_type=F32)


def to_column(lanes, count, start=0):
    shape = (count, lanes.shape[1])
    return jnp.sum(jnp.where(iota(shape, 1) == iota(shape, 0) + start, lanes, 0.0), axis=1, keepdims=True)


def to_lanes(column, start=0, width=128):
    shape = (column.shape[0], width)
    return jnp.sum(jnp.where(iota(shape, 1) == iota(shape, 0) + start, column, 0.0), axis=0, keepdims=True)


def halves(v):
    total = v[:, :128]
    for n in range(128, v.shape[1], 128):
        total = total + v[:, n : n + 128]
    return total


def frame_masks(bounds, frames):
    last = bounds.shape[1] - 1

    def living(f):
        return (f >= 0) & (f < bounds[0, last])

    def paired(f):
        both = living(f) & living(f + 1)
        for k in range(1, last):
            both = both & (f + 1 != bounds[0, k])
        return both

    return tuple(m.astype(F32) for m in (living(frames), paired(frames - 1), paired(frames)))


def row_valid(row, rows):
    mel = lax.axis_index("mel") * rows + row
    return ((mel >= 0) & (mel < lax.axis_size("mel") * rows)).astype(F32)


def start_all(*pairs, sems):
    copies = [pltpu.make_async_copy(src, dst, sems.at[n]) for n, (src, dst) in enumerate(pairs)]
    for copy in copies:
        copy.start()
    return copies


def wait_all(copies):
    for copy in copies:
        copy.wait()


def shifted_frames(value, behind, ahead):
    wide = value.shape[1]
    return pltpu.roll(value, 1, 1) * behind, pltpu.roll(value, wide - 1, 1) * ahead


def three_parts(v):
    high = lax.reduce_precision(v, 8, 7)
    mid = lax.reduce_precision(v - high, 8, 7)
    return high, mid, v - high - mid


def share_of(devices, chan):
    return -(-chan // devices)


def pack(spec_hbm, grad_hbm, bounds_hbm, out, own, spec, masks, bounds, edges, rows_out, sems):
    copies = start_all((bounds_hbm, bounds), (spec_hbm, spec), (grad_hbm, own), sems=sems)
    copies[0].wait()
    wide = masks.shape[1]
    frame_dev = wide - RIM
    devices = out.shape[0]
    rows = MEL_ROWS
    lane = iota((1, wide), 1)
    frames = lax.axis_index("tm") * frame_dev + jnp.where(lane < frame_dev + RIM // 2, lane, lane - wide)
    last = bounds.shape[1] - 1
    pixels = (bounds[0, last] * (lax.axis_size("mel") * rows)).astype(F32)
    found = frame_masks(bounds, frames)
    masks[...] = jnp.concatenate(
        list(found) + [jnp.full((1, wide), 1.0) * pixels, jnp.zeros((4, wide), F32)], axis=0
    )
    usable, behind, ahead = (m[:, :frame_dev] for m in found)
    copies[1].wait()
    x = spec[0].astype(F32) * usable
    lane = iota((1, frame_dev), 1)
    row = iota((rows, 1), 0)
    inner = jnp.where((lane > 0) & (lane < frame_dev - 1), usable, 0.0)
    number = (rows - 2) * jnp.sum(inner, axis=1, keepdims=True)
    inner = inner * ((row > 0) & (row < rows - 1)).astype(F32)
    centre = jnp.sum(jnp.sum(x, axis=0, keepdims=True), axis=1, keepdims=True)
    centre = centre / (rows * jnp.maximum(jnp.sum(usable, axis=1, keepdims=True), 1.0))
    centre = lax.reduce_precision(centre, 8, 7)
    shifted = [pltpu.roll(x, 1, 1) * behind, x, pltpu.roll(x, frame_dev - 1, 1) * ahead]
    taps = [pltpu.roll(v, (1 - i) % rows, 0) if i != 1 else v for i in range(3) for v in shifted]
    features = feature_rows(centre, (taps, inner))
    lane = iota((1, 128), 1)
    features = jnp.where(lane == 90, centre, jnp.where(lane == 91, number, features))
    pick = iota((8, frame_dev), 0)
    column = jnp.where(pick < 4, pick, frame_dev - 8 + pick)
    strip = dot((iota((8, frame_dev), 1) == column).astype(BF16), x.astype(BF16), ((1,), (1,)))
    lane = iota((8, 128), 1)
    repeat = (iota((rows, 128), 1) % rows == iota((rows, 128), 0)).astype(BF16)
    strip = jnp.where(lane // rows == iota((8, 128), 0), dot(strip.astype(BF16), repeat), 0.0)
    strip = jnp.sum(strip, axis=0, keepdims=True)

    def put(n, value):
        rows_out[pl.ds(n, devices, stride=FIRST), :] = jnp.broadcast_to(value, (devices, 128))

    near = jnp.concatenate([x[0:2], x[rows - 2 :]], axis=0)
    near = jnp.concatenate([near[:, :128], near[:, 128:]], axis=0)
    for d in range(devices):
        rows_out[FIRST * d : FIRST * d + 8, :] = near
    put(COLUMNS, strip)
    copies[2].wait()
    _, chan, many, half = own.shape
    share = share_of(devices, chan)
    holders = chan // share
    g = own[0].astype(F32)
    edges[0:chan] = g[:, 0, :]
    edges[chan:] = g[:, many - 1, :]

    def spread_out(v, held):
        if held < devices:
            v = jnp.concatenate([v, jnp.zeros((devices - held, 128), F32)], axis=0)
        return v

    for n in range(share):
        put(EDGES + n, spread_out(edges[n * holders : (n + 1) * holders, :], holders))
        put(EDGES + share + n, spread_out(edges[chan + n * holders : chan + (n + 1) * holders, :], holders))
    for n in range(2 * share, COLUMNS - EDGES):
        put(EDGES + n, jnp.zeros((1, 128), F32))
    end = iota((8, half), 0)
    at = iota((8, half), 1)
    ends = ((end == 0) & (at == 0)) | ((end == 1) & (at == half - 1))
    columns = dot(ends.astype(BF16), g.reshape(chan * many, half).astype(BF16), ((1,), (1,)))
    group = 128 // many
    source = iota((128, 128), 0)
    lane = iota((group, 128), 1)
    mine = lane // many == iota((group, 128), 0)
    lane8, own8 = iota((8, 128), 1), iota((8, 128), 0)
    parts = three_parts(features)
    for n in range(2):
        side = jnp.zeros((holders, 128), F32)
        for m in range(share):
            move = (iota((128, 128), 1) == SIDE + many * m + source % many).astype(BF16)
            first = m * holders * many // 128
            block = [columns[n : n + 1, 128 * q : 128 * (q + 1)] for q in range(first, first + holders * many // 128)]
            block = jnp.concatenate([jnp.where(mine, v, 0.0) for v in block], axis=0)
            side = side + dot(block.astype(BF16), move)
        far = x[2:4] if n == 0 else x[rows - 4 : rows - 2]
        pieces = [far[r : r + 1, 128 * h : 128 * (h + 1)] for r in range(2) for h in range(2)]
        pieces = jnp.concatenate([jnp.where(lane8 // 16 == own8, v, 0.0) for v in pieces], axis=0)
        far = dot(pieces.astype(BF16), (iota((128, 128), 1) == FAR + source % 16).astype(BF16))
        put(SUMS + n, spread_out(side, holders) + spread_out(far, FAR_HOLDERS) + parts[n])
    put(SUMS + 2, parts[2])
    out[...] = rows_out[...].reshape(out.shape).astype(BF16)


def weights(own, bounds_hbm, k2_hbm, k1_hbm, gain_one_hbm, bias_one_hbm, gain_two_hbm, bias_two_hbm,
            wf, wb, w1, ws_hbm, pairs, singles, k1t, params, all_masks, edge_masks, twice, own_rows,
            k2, k1, vectors, bounds, ws, temp, sems):
    loads = start_all(
        (bounds_hbm, bounds),
        (k2_hbm, k2),
        (k1_hbm, k1),
        (gain_one_hbm, vectors.at[0]),
        (bias_one_hbm, vectors.at[1]),
        (gain_two_hbm, vectors.at[2]),
        (bias_two_hbm, vectors.at[3]),
        sems=sems,
    )
    _, many, count, half = own.shape
    temp[...] = own[0].astype(F32).reshape(many * count, half)
    for r in range(count):
        own_rows[r * many : (r + 1) * many] = temp[pl.ds(r, many, stride=count), :].astype(BF16)
    wait_all(loads)
    chan = k2.shape[1]
    span = wf.shape[1]
    taps = [k2[t].astype(F32) for t in range(9)]
    rest = jnp.zeros((chan, span - 9 * chan), F32)
    forward = jnp.concatenate(taps + [rest], axis=1)
    backward = jnp.concatenate([taps[8 - t].T for t in range(9)] + [rest], axis=1)
    for r in range(wb.shape[0] // chan):
        at = slice(r * chan, (r + 1) * chan)
        wb[at] = (pltpu.roll(backward, 3 * chan * r, 1) if r else backward).astype(BF16)
    full = jnp.concatenate([k1[n].astype(F32) for n in range(3)] + [jnp.zeros((7, chan), F32)], axis=0)
    low = [
        jnp.concatenate([full[3 * (2 - a) + 2 - b : 3 * (2 - a) + 3 - b] for a in range(3)], axis=1)
        for b in range(3)
    ]
    rest = jnp.zeros((1, ws.shape[1] - 3 * chan), F32)
    for b in range(3):
        base = jnp.concatenate([low[b], rest], axis=1)
        many = ws.shape[0] // 3
        rolled = [pltpu.roll(base, chan * m, 1) if m else base for m in range(many)]
        ws[many * b : many * (b + 1)] = jnp.concatenate(rolled, axis=0).astype(BF16)
    store_ws = pltpu.make_async_copy(ws, ws_hbm, sems.at[7])
    store_ws.start()
    count, frame_dev = all_masks.shape[0] // 3, all_masks.shape[1]
    frames = iota((count, frame_dev), 0) * frame_dev + iota((count, frame_dev), 1)
    for n, mask in enumerate(frame_masks(bounds, frames)):
        all_masks[n * count : (n + 1) * count] = mask
    q = iota(edge_masks.shape, 0)
    lane = iota(edge_masks.shape, 1)
    k = q % 8
    frames = (q // 8) * frame_dev + jnp.where(k < 4, k, k + frame_dev - 8)
    living, behind, ahead = frame_masks(bounds, frames)
    living = jnp.where((k == 0) | (k == 7), living, 0.0)
    edge_masks[...] = jnp.where(lane == 0, living, jnp.where(lane == 1, behind, jnp.where(lane == 2, ahead, 0.0)))
    params[...] = jnp.concatenate(
        [vectors[n] for n in range(4)] + [jnp.zeros((4, chan), F32)], axis=0
    )
    tap = iota((16, 128), 0)
    lane = iota((16, 128), 1)
    i = (tap * 11) >> 5
    ninth = (lane * 57) >> 9
    to_band = (lane == BAND * (tap - 3 * i) + i) & (tap < 9)
    to_left = (ninth == tap) & (tap < 9)
    to_right = (lane - 9 * ninth == tap) & (lane < 81)
    to_single = (lane == 81 + tap) & (tap < 9)
    source = iota((128, 128), 0) - 81
    lane = iota((128, 128), 1)
    ninth = (lane * 57) >> 9
    inside = (source >= 0) & (source < 9) & (lane < 81)
    twice[...] = jnp.where(inside, (source == ninth).astype(F32) + (source == lane - 9 * ninth).astype(F32), 0.0)
    for r in range(wf.shape[0] // chan):
        at = slice(r * chan, (r + 1) * chan)
        wf[at] = (pltpu.roll(forward, 3 * chan * r, 1) if r else forward).astype(BF16)
    k1t[...] = full
    k = full.astype(BF16)
    lanes = [dot(k, select.astype(BF16), ((0,), (0,))) for select in (to_band, to_left, to_right, to_single)]
    pairs[...] = lanes[1] * lanes[2]
    singles[...] = lanes[3]
    for m in range(w1.shape[0] // chan):
        w1[m * chan : (m + 1) * chan] = (pltpu.roll(lanes[0], m, 1) if m else lanes[0]).astype(BF16)
    store_ws.wait()


def feature_rows(centre, *parts):
    def folded(v):
        return jnp.sum(halves(v), axis=0, keepdims=True)

    rows = [jnp.zeros((1, 128), F32)] * 96
    for taps, weight in parts:
        z = [tap - centre for tap in taps]
        for s in range(9):
            left = z[s] * weight
            rows[81 + s] = rows[81 + s] + folded(left)
            for t in range(s, 9):
                rows[9 * s + t] = rows[9 * t + s] = rows[9 * s + t] + folded(left * z[t])
    return to_lanes(jnp.sum(jnp.concatenate(rows, axis=0), axis=1, keepdims=True))


def summed_blocks(ref, devices, by=1):
    block = ref.shape[0] // devices
    period = max(8 // math.gcd(block, 8), by)
    step = period * block
    total = ref[0:step, :]
    for at in range(step, ref.shape[0], step):
        total = total + ref[at : at + step, :]
    results = []
    for first in range(by):
        result = total[first * block : (first + 1) * block]
        for n in range(first + by, period, by):
            result = result + total[n * block : (n + 1) * block]
        results.append(result)
    return results if by > 1 else results[0]


def moved_rows(v, step):
    if step == 0:
        return v
    count = v.shape[0]
    if abs(step) >= count:
        return jnp.zeros_like(v)
    zero = jnp.zeros((abs(step), v.shape[1]), v.dtype)
    if step > 0:
        return jnp.concatenate([zero, v[: count - step]], axis=0)
    return jnp.concatenate([v[-step:], zero], axis=0)


def silu_halves(h):
    t = jnp.tanh(h)
    one = 1.0 + t
    return h * one, one * (1.0 + h * (1.0 - t))


def act_row(act, r, low, low_masks):
    low = low * low_masks[0]
    chan = low.shape[0]
    for n, v in enumerate((low,) + shifted_frames(low, *low_masks[1:])):
        at = (3 * r + (1, 0, 2)[n]) * chan
        act[at : at + chan, :] = v


def forward_one(recv, spec, pairs, singles, twice, w1, wf, params, masks, all_masks, edge_masks,
                pre_two, payload, act, x3, far_rim, stats, features_out, pre_one, got, strips, halo, rows_out):
    devices = recv.shape[0]
    n_mel, count = lax.axis_size("mel"), lax.axis_size("tm")
    rows = MEL_ROWS
    mels = n_mel * rows
    wide = masks.shape[1]
    frame_dev = wide - RIM
    chan = params.shape[1]
    me_m, me_t = lax.axis_index("mel"), lax.axis_index("tm")
    usable, behind, ahead = (masks[n : n + 1] for n in range(3))
    total = masks[3:4, 0:1]
    got[...] = recv[...].astype(F32).reshape(devices * FIRST, 128)

    def every(n):
        return got[pl.ds(n, devices, stride=FIRST), :]

    lane = iota((count, 128), 1)
    bands = [got[pl.ds(FIRST * k * count + COLUMNS, count, stride=FIRST), :] for k in range(n_mel)]
    for c in range(8):
        column = jnp.zeros((count, 128), F32)
        for k, band in enumerate(bands):
            part = jnp.where(lane // rows == c, band, 0.0)
            column = column + (pltpu.roll(part, rows * (k - c) % 128, 1) if k != c else part)
        strips[pl.ds(c, count, stride=8), :] = column
    at = pl.multiple_of(FIRST * (jnp.maximum(me_m - 1, 0) * count + me_t), 8)
    above = got[pl.ds(at, 8), :] * (me_m > 0).astype(F32)
    at = pl.multiple_of(FIRST * (jnp.minimum(me_m + 1, n_mel - 1) * count + me_t), 8)
    below = got[pl.ds(at, 8), :] * (me_m < n_mel - 1).astype(F32)
    above = jnp.concatenate([above[2:4], above[6:8]], axis=1)
    below = jnp.concatenate([below[0:2], below[4:6]], axis=1)
    own = spec[0].astype(F32) * usable[:, :frame_dev]
    at = pl.multiple_of(8 * jnp.minimum(me_t + 1, count - 1), 8)
    after = strips[pl.ds(at, 8), :][:, :mels] * (me_t + 1 < count).astype(F32)
    at = pl.multiple_of(8 * jnp.maximum(me_t - 1, 0), 8)
    before = strips[pl.ds(at, 8), :][:, :mels] * (me_t > 0).astype(F32)
    sides = jnp.concatenate([after[0:4], before[4:8], jnp.zeros((8, mels), F32)], axis=0).astype(BF16)
    side = iota((16, RIM), 0)
    place = iota((16, RIM), 1) == jnp.where(side < 4, side, jnp.where(side < 8, side + RIM - 8, -1))
    halo[0:8] = jnp.zeros((8, RIM), F32)
    halo[mels : mels + 8] = jnp.zeros((8, RIM), F32)
    halo[4 : mels + 4] = dot(sides, place.astype(BF16), ((0,), (0,)))
    rim = halo[pl.ds(pl.multiple_of(me_m * rows, 8), BAND), :]
    far_rim[...] = rim
    row = iota((BAND, RIM), 0)
    rim = jnp.where((row >= 2) & (row < BAND - 2), rim, 0.0)
    blank = jnp.zeros((2, frame_dev), F32)
    near = jnp.concatenate([jnp.concatenate([blank, above, own, below, blank], axis=0), rim], axis=1)
    x3[...] = jnp.concatenate(
        [
            pltpu.roll(near, 1, 1) * behind,
            near,
            pltpu.roll(near, wide - 1, 1) * ahead,
            jnp.broadcast_to(usable, (BAND, wide)),
            jnp.zeros((128 - 4 * BAND, wide), F32),
        ],
        axis=0,
    ).astype(BF16)
    pre_one[2 * chan : (rows + 4) * chan] = dot(w1[2 * chan : (rows + 4) * chan, :], x3[...])
    lane = iota((1, 128), 1)
    parts = jnp.where(lane < 92, every(SUMS) + every(SUMS + 1) + every(SUMS + 2), 0.0)
    centres, numbers = parts[:, 90:91], parts[:, 91:92]
    centre = jnp.sum(centres * numbers, axis=0, keepdims=True)
    centre = centre / jnp.maximum(jnp.sum(numbers, axis=0, keepdims=True), 1.0)
    delta = centres - centre
    features = jnp.sum(parts + delta * numbers * jnp.where(lane < 81, delta, 1.0), axis=0, keepdims=True)
    moved = jnp.sum(delta * parts, axis=0, keepdims=True)
    def edge_row(k, n):
        first = FIRST * k * count + n
        return jnp.concatenate(
            [got[pl.ds(first, count, stride=FIRST), :], got[pl.ds(first + 4, count, stride=FIRST), :]], axis=1
        )

    edge_rows = [[edge_row(k, n) for n in range(4)] for k in range(n_mel)]
    zero = jnp.zeros((count, frame_dev), F32)
    rows_of = [[], [], []]
    for k, (top, second, fore, bottom) in enumerate(edge_rows):
        for n, v in enumerate((edge_rows[k - 1][3] if k else zero, top, second)):
            rows_of[n].append(v)
        for n, v in enumerate((fore, bottom, edge_rows[k + 1][0] if k + 1 < n_mel else zero)):
            rows_of[n].append(v)
    f_usable, f_behind, f_ahead = (all_masks[n * count : (n + 1) * count, :] for n in range(3))
    lane = iota((count, frame_dev), 1)

    def frame_before(v):
        v = pltpu.roll(v, 1, 1)
        return jnp.where(lane == 0, pltpu.roll(v, 1, 0), v) * f_behind

    def frame_after(v):
        v = pltpu.roll(v, frame_dev - 1, 1)
        return jnp.where(lane == frame_dev - 1, pltpu.roll(v, count - 1, 0), v) * f_ahead

    taps = []
    for group in rows_of:
        for move in (frame_before, lambda v: v, frame_after):
            taps.append(jnp.concatenate([move(v) for v in group], axis=1))
    f_usable = jnp.concatenate([f_usable] * (2 * n_mel), axis=1)
    borders = (taps, f_usable)
    edge = strips[...]
    q_usable, q_behind, q_ahead = (edge_masks[:, n : n + 1] for n in range(3))
    lane = iota((count * 8, 128), 1)
    inside = (lane < mels) & (lane % rows != 0) & (lane % rows != rows - 1)
    shifted = [
        pltpu.roll(edge, 1, 0) * q_behind,
        edge,
        pltpu.roll(edge, count * 8 - 1, 0) * q_ahead,
    ]
    taps = [pltpu.roll(v, (1 - i) % 128, 1) if i != 1 else v for i in range(3) for v in shifted]
    features = features + feature_rows(centre, borders, (taps, jnp.where(inside, q_usable, 0.0)))
    features = jnp.where(iota((1, 128), 1) < 90, features, 0.0)
    near_mean = jnp.sum(singles[...] * features, axis=1, keepdims=True) / total
    around = jnp.sum(singles[...], axis=1, keepdims=True)
    square = jnp.sum(pairs[...] * features, axis=1, keepdims=True)
    square = (square + 2.0 * around * jnp.sum(singles[...] * moved, axis=1, keepdims=True)) / total
    inv = lax.rsqrt(square - near_mean * near_mean + 1e-05)
    mean = near_mean + centre * around
    lane = iota((chan, 128), 1)
    stats[0:chan] = jnp.where(lane == 0, mean, jnp.where(lane == 1, inv, 0.0))
    stats[chan : chan + 8] = jnp.broadcast_to(to_lanes(near_mean), (8, 128))
    stats[chan + 8 : chan + 16] = jnp.broadcast_to(to_lanes(inv), (8, 128))
    scale = 0.5 * to_column(params[0:1], chan) * inv
    shift = 0.5 * to_column(params[1:2], chan) - mean * scale
    stats[chan + 16 :] = jnp.where(lane == 0, scale, jnp.where(lane == 1, shift, 0.0))
    scale = jnp.broadcast_to(scale, (chan, wide))
    shift = jnp.broadcast_to(shift, (chan, wide))
    block, taps = wf.shape
    first = jnp.zeros((chan, 128), F32)
    second = jnp.zeros((chan, 128), F32)
    own_mask = usable[:, :frame_dev]
    low_masks = [m.astype(BF16) for m in (usable, behind, ahead)]
    for r in range(2, rows + 4):
        value, _ = silu_halves(pre_one[r * chan : (r + 1) * chan, :] * scale + shift)
        if not 0 <= r - 3 < rows:
            value = value * row_valid(r - 3, rows)
        act_row(act, r, value.astype(BF16), low_masks)
        if r < 5 or r % 2 == 0:
            continue
        g = (r - 3) // 2
        result = dot(wf[...], act[g * 3 * block : g * 3 * block + taps, :frame_dev])
        at = (g - 1) * block
        pre_two[at : at + block, :frame_dev] = result
        if g % 2 == 0:
            beside = [act[n * 3 * block : n * 3 * block + taps, frame_dev:] for n in (g - 1, g)]
            beside = dot(wf[...], jnp.concatenate(beside, axis=1))
            for n in range(2):
                pre_two[at + (n - 1) * block : at + n * block, frame_dev:] = beside[:, n * RIM : (n + 1) * RIM]
        for q in range(2):
            p = result[q * chan : (q + 1) * chan]
            masked = p * own_mask
            first = first + halves(masked)
            second = second + halves(masked * p)
    moved = dot(jnp.broadcast_to(moved, (8, 128)), twice[...], precision=EXACT)[0:1]
    features_out[...] = jnp.concatenate(
        [features + moved, jnp.broadcast_to(centre, (1, 128)), jnp.zeros((6, 128), F32)], axis=0
    )
    share = share_of(devices, chan)

    def put(n, value):
        rows_out[pl.ds(n, devices, stride=SECOND), :] = jnp.broadcast_to(value, (devices, 128))

    for n in range(share):
        put(3 + n, moved_rows(every(EDGES + share + n), count))
        put(3 + share + n, moved_rows(every(EDGES + n), -count))
    for n in [0, 1, 2] + list(range(3 + 2 * share, SECOND - 1)):
        put(n, jnp.zeros((1, 128), F32))
    lane = iota((devices, 128), 1)
    tm = iota((devices, 128), 0) % count
    at_side = (lane >= SIDE) & (lane < FAR)
    lefts = jnp.where(at_side, every(SUMS), 0.0)
    rights = jnp.where(at_side, every(SUMS + 1), 0.0)
    beside = jnp.zeros((devices, 128), F32)
    for n, step in enumerate((0, count, -count)):
        one = jnp.where(tm > 0, moved_rows(rights, step + 1), 0.0)
        two = jnp.where(tm < count - 1, moved_rows(lefts, step - 1), 0.0)
        beside = beside + pltpu.roll(one, (32 * n - SIDE) % 128, 1) + pltpu.roll(two, (32 * n + 16 - SIDE) % 128, 1)
    outer = jnp.where(lane >= FAR, moved_rows(every(SUMS + 1), count), 0.0)
    beside = beside + pltpu.roll(outer, 128 - 16, 1)
    beside = beside + jnp.where(lane >= FAR, moved_rows(every(SUMS), -count), 0.0)
    put(SECOND - 1, beside)
    first = jnp.sum(first, axis=1, keepdims=True)
    second = jnp.sum(second, axis=1, keepdims=True)
    parts = list(three_parts(to_lanes(first) + to_lanes(second, chan)))
    parts = jnp.concatenate(parts + [jnp.zeros((SECOND - 3, 128), F32)], axis=0)
    for d in range(devices):
        payload[d] = (rows_out[SECOND * d : SECOND * (d + 1), :] + parts).astype(BF16)


def spreading(half):
    lane = iota((half, 2 * half), 1)
    return jnp.where(lane >> 1 == iota((half, 2 * half), 0), 0.25, 0.0).astype(BF16)


def half_share(devices, taps):
    return -(-taps // 2 // devices)


def backward_scaled(recv, pre_two, act, own_rows, params, masks,
                    grad, kept_half, sent_half, totals, stats, up, right, got, halved):
    devices = recv.shape[0]
    got[...] = recv[:, 0:SECOND, :].astype(F32).reshape(devices * SECOND, 128)
    chan = params.shape[1]
    half = own_rows.shape[1]
    frame_dev = 2 * half
    rows = MEL_ROWS
    up[...] = dot(own_rows[...], spreading(half))
    usable = masks[0:1, :frame_dev]
    total = masks[3:4, 0:1]
    sums = [got[pl.ds(n, devices, stride=SECOND), :] for n in range(3)]
    sums = jnp.sum(sums[0] + sums[1] + sums[2], axis=0, keepdims=True)
    mean = to_column(sums, chan) / total
    inv = lax.rsqrt(to_column(sums, chan, chan) / total - mean * mean + 1e-05)
    scale = 0.5 * to_column(params[2:3], chan) * inv
    shift = 0.5 * to_column(params[3:4], chan) - mean * scale
    lane = iota((chan, 128), 1)
    columns = jnp.zeros((chan, 128), F32)
    for n, column in enumerate((mean, inv, scale, shift)):
        columns = jnp.where(lane == n, column, columns)
    stats[0:chan] = columns
    stats[chan : chan + 8] = jnp.broadcast_to(to_lanes(inv), (8, 128))
    mean, inv, scale, shift = (jnp.broadcast_to(v, (chan, frame_dev)) for v in (mean, inv, scale, shift))
    first = jnp.zeros((chan, 128), F32)
    second = jnp.zeros((chan, 128), F32)
    mask = 0.5 * usable
    right[3 * chan :] = jnp.ones((16, rows * frame_dev), BF16)
    table = jnp.zeros((9 * chan, 3 * chan + 16), F32)
    for m in range(rows):
        at = slice(m * chan, (m + 1) * chan)
        pre = pre_two[at, :frame_dev]
        _, slope = silu_halves(pre * scale + shift)
        g = up[m // 2 * chan : (m // 2 + 1) * chan, :] * slope * mask
        grad[at, :] = g
        normed = (pre - mean) * inv
        first = first + halves(g * normed)
        second = second + halves(g)
        lanes = slice(m * frame_dev, (m + 1) * frame_dev)
        right[0:chan, lanes] = g.astype(BF16)
        right[chan : 2 * chan, lanes] = normed.astype(BF16)
        right[2 * chan : 3 * chan, lanes] = (g - right[0:chan, lanes].astype(F32)).astype(BF16)
        if m in (5, 11, rows - 1):
            start = m - m % 6
            left = [act[(n + 2) * 3 * chan : (n + 5) * 3 * chan, :frame_dev] for n in range(start, m + 1)]
            lanes = slice(start * frame_dev, (m + 1) * frame_dev)
            table = table + dot(jnp.concatenate(left, axis=1), right[:, lanes], ((1,), (1,)))
    first = jnp.sum(first, axis=1, keepdims=True)
    second = jnp.sum(second, axis=1, keepdims=True)
    totals[...] = jnp.broadcast_to(to_lanes(first) + to_lanes(second, chan), (8, 128))
    rest = jnp.concatenate([table[:, 2 * chan :], jnp.zeros((9 * chan, chan - 16), F32)], axis=1)
    both = table[:, : 2 * chan] + jnp.where(iota(rest.shape, 1) < chan, rest, 0.0)
    single = rest[:, chan : chan + 1]
    taps = 9 * chan // 2
    lane = iota((devices, 128), 1)
    for h in range(2):
        halved[h, 0:taps] = both[h * taps : (h + 1) * taps]
        constants = jnp.zeros((devices, 128), F32)
        for k in range(half_share(devices, 9 * chan)):
            at = h * taps + k * devices
            ones = single[at : min(at + devices, (h + 1) * taps)]
            if ones.shape[0] < devices:
                ones = jnp.concatenate([ones, jnp.zeros((devices - ones.shape[0], 1), F32)], axis=0)
            constants = jnp.where(lane == k, ones, constants)
        halved[h, taps:] = constants
    core = lax.axis_index("tm") % 2
    kept_half[...] = halved[core]
    sent_half[...] = halved[1 - core]


def around(recv, pre_two, act, w1, wf, x3, far_rim, stats_one, masks, stats, pre_ring, ring, rim, pairs,
           sides, up, got, beyond, more):
    devices = recv.shape[0]
    got[...] = recv[:, 0:SECOND, :].astype(F32).reshape(devices * SECOND, 128)
    rows = MEL_ROWS
    many = rows // 2
    wide = pre_two.shape[1]
    frame_dev = wide - RIM
    chan = pre_two.shape[0] // rows
    usable = masks[0:1]
    low_masks = [masks[n : n + 1].astype(BF16) for n in range(3)]
    pieces = got[pl.ds(SECOND - 1, devices, stride=SECOND), :][:FAR_HOLDERS].astype(BF16)
    source = iota((128, 128), 0)
    lane = iota((FAR_HOLDERS, 128), 1)
    mine = lane // 16 == iota((FAR_HOLDERS, 128), 0) % 8
    outer = []
    for first in (SIDE, FAR):
        place = (source - first == iota((128, 128), 1) % 16).astype(BF16)
        v = jnp.where(mine, dot(pieces, place), 0.0)
        v = [jnp.sum(v[8 * n : 8 * n + 8], axis=0, keepdims=True) for n in range(4)]
        outer += [jnp.concatenate(v[2 * r : 2 * r + 2], axis=1) for r in range(2)]
    blank = jnp.zeros((BAND - 4, frame_dev), F32)
    far = jnp.concatenate(outer[:2] + [blank] + outer[2:], axis=0)
    row = iota((BAND, RIM), 0)
    far = jnp.concatenate([far, jnp.where((row < 2) | (row >= BAND - 2), far_rim[...], 0.0)], axis=1)
    far = jnp.concatenate(
        [
            pltpu.roll(far, 1, 1) * masks[1:2],
            far,
            pltpu.roll(far, wide - 1, 1) * masks[2:3],
            jnp.zeros((128 - 3 * BAND, wide), F32),
        ],
        axis=0,
    )
    x_all = (x3[...].astype(F32) + far).astype(BF16)
    scale = jnp.broadcast_to(stats_one[chan + 16 :, 0:1], (chan, wide))
    shift = jnp.broadcast_to(stats_one[chan + 16 :, 1:2], (chan, wide))
    for h, start in enumerate((0, rows + 4)):
        pre_one = dot(w1[start * chan : (start + 2) * chan, :], x_all)
        for n in range(2):
            value, _ = silu_halves(pre_one[n * chan : (n + 1) * chan] * scale + shift)
            value = value * row_valid(start + n - 3, rows)
            act_row(more, 2 * h + n, value.astype(BF16), low_masks)
    line = 3 * chan
    above = jnp.concatenate([more[0 : 2 * line, :], act[2 * line : 4 * line, :]], axis=0)
    below = jnp.concatenate([act[(rows + 2) * line : (rows + 4) * line, :], more[2 * line :, :]], axis=0)
    pre_ring[0 : 2 * chan] = dot(wf[...], above)
    pre_ring[2 * chan :] = dot(wf[...], below)
    share = share_of(devices, chan)
    holders = chan // share

    def every(n):
        return got[pl.ds(n, devices, stride=SECOND), :]

    beside = every(SECOND - 1)[:holders]
    lane = iota((holders, RIM), 1)
    for n in range(share):
        first = n * holders
        beyond[first : first + holders, :] = every(3 + n)[:holders]
        beyond[chan + first : chan + first + holders, :] = every(3 + share + n)[:holders]
        for r in range(many + 2):
            at = many * n + (r if r < many else 32 + many - 1 if r == many else 64)
            left, right_of = beside[:, at : at + 1], beside[:, at + 16 : at + 17]
            side = jnp.where(lane >= RIM - 2, 0.25 * left, jnp.where(lane < 2, 0.25 * right_of, 0.0))
            sides[r * chan + first : r * chan + first + holders, :] = side
    up[...] = dot(beyond[...].astype(BF16), spreading(frame_dev // 2))
    scale = jnp.broadcast_to(stats[0:chan, 2:3], (chan, wide))
    shift = jnp.broadcast_to(stats[0:chan, 3:4], (chan, wide))
    for n, m in enumerate((-2, -1, rows, rows + 1)):
        below = n // 2
        upstream = jnp.concatenate(
            [
                up[below * chan : (below + 1) * chan, :],
                sides[(many + below) * chan : (many + below + 1) * chan, :],
            ],
            axis=1,
        )
        _, slope = silu_halves(pre_ring[n * chan : (n + 1) * chan, :] * scale + shift)
        ring[n * chan : (n + 1) * chan, :] = upstream * slope * (usable * (0.5 * row_valid(m, rows)))
    both = None
    for m in range(rows):
        at = slice(m * chan, (m + 1) * chan)
        _, slope = silu_halves(pre_two[at, frame_dev:] * scale[:, frame_dev:] + shift[:, frame_dev:])
        upstream = sides[m // 2 * chan : (m // 2 + 1) * chan, :]
        rim[m * chan : (m + 1) * chan, :] = upstream * slope * (0.5 * usable[:, frame_dev:])
        value, _ = silu_halves(pre_two[at, :frame_dev] * scale[:, :frame_dev] + shift[:, :frame_dev])
        value = value * usable[:, :frame_dev]
        both = value if m % 2 == 0 else both + value
        if m % 2:
            pairs[m // 2 * chan : (m // 2 + 1) * chan, :] = both


def pack_sums(kept_half, received, totals, after, payload):
    del after
    devices = kept_half.shape[0] - TAPS // 2
    block = payload.shape[0] // devices
    payload[pl.ds(0, devices, stride=block), :] = jnp.broadcast_to(totals[0:1], (devices, 128))
    taps = TAPS // 2
    total = kept_half[...] + received[...]
    for k in range(block - 2):
        cut = total[k * devices : min((k + 1) * devices, taps)]
        if cut.shape[0] < devices:
            cut = jnp.concatenate([cut, jnp.zeros((devices - cut.shape[0], 128), F32)], axis=0)
        payload[pl.ds(1 + k, devices, stride=block), :] = cut
    payload[pl.ds(block - 1, devices, stride=block), :] = total[taps:]


def pool(totals, pairs, out, gain_out, bias_out, temp):
    gain_out[...] = totals[0:1, : gain_out.shape[1]]
    bias_out[...] = totals[0:1, gain_out.shape[1] :]
    chan, rows, half = out.shape[1:]
    to_mean = jnp.where(iota((2 * half, half), 0) >> 1 == iota((2 * half, half), 1), 0.25, 0.0)
    pooled = dot(pairs[...], to_mean, precision=EXACT)
    for r in range(rows):
        temp[pl.ds(r, chan, stride=rows), :] = pooled[r * chan : (r + 1) * chan]
    out[0] = temp[...].reshape(chan, rows, half).astype(BF16)


def backward(recv, pre_two, pre_ring, grad, ring, rim, stats_two, w1, x3, stats, params, masks, wb,
             out, own_low, payload, totals, g3, pre_one, g1):
    chan = params.shape[1]
    rows = MEL_ROWS
    wide = pre_two.shape[1]
    frame_dev = wide - RIM
    usable = masks[0:1]
    behind, ahead = (masks[n : n + 1].astype(BF16) for n in (1, 2))
    total = masks[3:4, 0:1]
    devices = payload.shape[0] // 14
    pre_one[...] = dot(w1[3 * chan : (rows + 3) * chan], x3[:, :frame_dev])

    even, odd = summed_blocks(recv, devices, 2)
    sums = even[0:1] + odd[0:1]
    gain_sum, bias_sum = sums[:, :chan], sums[:, chan:]
    totals[...] = jnp.broadcast_to(sums, (8, 128))
    mean, inv = stats_two[0:chan, 0:1], stats_two[0:chan, 1:2]
    factor = to_column(params[2:3], chan) * inv
    gain_part = factor * (to_column(sums, chan) / total * inv)
    bias_part = factor * (to_column(sums, chan, chan) / total) - mean * gain_part
    gain_part = jnp.broadcast_to(gain_part, (chan, wide))
    bias_part = jnp.broadcast_to(bias_part, (chan, wide))
    factor = jnp.broadcast_to(factor, (chan, wide))
    scale = jnp.broadcast_to(stats[chan + 16 :, 0:1], (chan, frame_dev))
    shift = jnp.broadcast_to(stats[chan + 16 :, 1:2], (chan, frame_dev))
    factor_one = jnp.broadcast_to(to_column(params[0:1], chan) * stats[0:chan, 1:2], (chan, frame_dev))
    own_mask = 0.5 * usable[:, :frame_dev]
    count = rows + 4
    share = even.shape[0] - 2
    mine = jnp.concatenate([even[1 : share + 1], odd[1 : share + 1]], axis=0)
    single = jnp.concatenate([to_column(v[share + 1 :], share) for v in (even, odd)], axis=0)
    factor_l = params[2:3] * stats_two[chan : chan + 1, :chan]
    mine = mine[:, :chan] - (bias_sum * single + gain_sum * mine[:, chan:]) / total
    mine = factor_l * mine
    mine = jnp.concatenate([mine[:share], mine[share:]], axis=1)
    if share < 9:
        mine = jnp.concatenate([mine, jnp.zeros((9 - share, 128), F32)], axis=0)
    table = jnp.zeros((chan, 128), F32)

    def tap_sums(m):
        part = g1[m * chan : (m + 4) * chan, :]
        high = lax.reduce_precision(part, 8, 7)
        low = (part - high).astype(BF16)
        taps_in = x3[:, :frame_dev]
        products = dot(high.astype(BF16), taps_in, ((1,), (1,))) + dot(low, taps_in, ((1,), (1,)))
        moved = [pltpu.roll(products[k * chan : (k + 1) * chan], 128 - (m + k + 3), 1) for k in range(4)]
        return (moved[0] + moved[1]) + (moved[2] + moved[3])

    for q in range(count):
        at = slice(q * chan, (q + 1) * chan)
        mask = usable if 0 <= q - 2 < rows else usable * row_valid(q - 2, rows)
        if 2 <= q < rows + 2:
            own = slice((q - 2) * chan, (q - 1) * chan)
            pre, scaled = pre_two[own, :], jnp.concatenate([grad[own, :], rim[own, :]], axis=1)
        else:
            n = q if q < 2 else q - rows
            pre, scaled = pre_ring[n * chan : (n + 1) * chan, :], ring[n * chan : (n + 1) * chan, :]
        low = (factor * scaled - (bias_part + pre * gain_part) * mask).astype(BF16)
        out[at, :] = low
        if not 1 <= q < count - 1:
            continue
        base = (q - 1) * 3 * chan
        for n, v in enumerate((low,) + shifted_frames(low, behind, ahead)):
            spot = base + (1, 0, 2)[n] * chan
            g3[spot : spot + chan, :] = v[:, :frame_dev]
        start = q - 4
        if start < 0 or start % 2:
            continue
        result = dot(wb[...], g3[start * 3 * chan : (start + 4) * 3 * chan, :])
        for n in range(2):
            m = start + n
            at = slice(m * chan, (m + 1) * chan)
            _, slope = silu_halves(pre_one[at, :] * scale + shift)
            value = result[n * chan : (n + 1) * chan] * slope * own_mask
            own_low[at, :] = (value * factor_one).astype(BF16)
            g1[at, :] = value
        if start % 4 == 2 and start > 2:
            table = table + tap_sums(start - 6)
    table = table + tap_sums(rows - 4)
    table = table.T
    places = [BAND * j + i for i in range(3) for j in range(3)] + [3 * BAND]
    rows10 = jnp.concatenate([table[n : n + 1] for n in places], axis=0)
    sums = jnp.concatenate([rows10[0:5], rows10[5:10]], axis=1)
    block = jnp.concatenate([sums, mine], axis=0)
    block = jnp.concatenate([block] * 4, axis=0)
    for d in range(0, devices, 4):
        payload[14 * d : 14 * (d + 4), :] = block


def transposed(grad, own_low, w1, wb, x3, stats, features, k1t, params, masks, ws_hbm,
               first, ws, normed_taps, low, g3, rim, sem):
    load = pltpu.make_async_copy(ws_hbm, ws, sem)
    load.start()
    rows = MEL_ROWS
    chan = own_low.shape[0] // rows
    wide = grad.shape[1]
    frame_dev = wide - RIM
    count = grad.shape[0] // chan
    usable = masks[0:1]
    behind, ahead = (masks[n : n + 1].astype(BF16) for n in (1, 2))
    scale = jnp.broadcast_to(stats[chan + 16 :, 0:1], (chan, wide))
    shift = jnp.broadcast_to(stats[chan + 16 :, 1:2], (chan, wide))
    factor = jnp.broadcast_to(to_column(params[0:1], chan) * stats[0:chan, 1:2], (chan, wide))
    edge = (0, 1, 2, 3, count - 4, count - 3, count - 2, count - 1)
    for q in range(count):
        value = grad[q * chan : (q + 1) * chan, :]
        for n, v in enumerate((value,) + shifted_frames(value, behind, ahead)):
            spot = (3 * q + (1, 0, 2)[n]) * chan
            rim[spot : spot + chan, :] = v[:, frame_dev:]
            if q in edge:
                spot = (3 * edge.index(q) + (1, 0, 2)[n]) * chan
                g3[spot : spot + chan, :] = v[:, :frame_dev]
    low[chan : (rows + 1) * chan, :frame_dev] = own_low[...]

    def put(m, lanes, result, pre_one):
        at = slice((m + 1) * chan, (m + 2) * chan)
        _, slope = silu_halves(pre_one * scale[:, lanes] + shift[:, lanes])
        mask = usable[:, lanes] * (0.5 * row_valid(m, rows))
        low[at, lanes] = (result * slope * mask * factor[:, lanes]).astype(BF16)

    pre_one = dot(w1[2 * chan : (rows + 4) * chan, :], x3[:, frame_dev:])
    beside = slice(frame_dev, wide)
    for start in range(0, rows + 2, 2):
        result = dot(wb[...], rim[start * 3 * chan : (start + 4) * 3 * chan, :])
        for n in range(2):
            at = slice((start + n) * chan, (start + n + 1) * chan)
            put(start + n - 1, beside, result[n * chan : (n + 1) * chan], pre_one[at])
    own = slice(0, frame_dev)
    result = dot(wb[...], g3[: 4 * 3 * chan, :])
    put(-1, own, result[:chan], dot(w1[2 * chan : 3 * chan, :], x3[:, :frame_dev]))
    result = dot(wb[...], g3[4 * 3 * chan :, :])
    put(rows, own, result[chan:], dot(w1[(rows + 3) * chan : (rows + 4) * chan, :], x3[:, :frame_dev]))
    row = features[0:1, :]
    lane = iota((1, 128), 1)
    gram = jnp.concatenate(
        [jnp.where(lane < 9, pltpu.roll(row, 128 - 9 * t, 1) if t else row, 0.0) for t in range(9)]
        + [jnp.zeros((7, 128), F32)],
        axis=0,
    )
    single = to_column(row, 16, 81)[0:9]
    k_rows = jnp.concatenate([k1t[...], jnp.zeros((112, chan), F32)], axis=0)
    mean_l, inv_l = stats[chan : chan + 1, :chan], stats[chan + 8 : chan + 9, :chan]
    normed = inv_l * (dot(gram, k_rows, precision=EXACT)[0:9] - single * mean_l)
    normed_taps[0:16] = jnp.concatenate([normed, jnp.zeros((7, chan), F32)], axis=0)
    normed_taps[16:32] = jnp.broadcast_to(to_column(row, 16, 81), (16, chan))
    load.wait()
    first[...] = dot(ws[...], low[...])


def finish(recv, features, stats, k1t, first, ws, w1, x3, normed_taps, params, masks,
           spec_hbm, kernel_one_hbm, kernel_two_hbm, gain_hbm, bias_hbm,
           spec_grad, kernel_one, kernel_two, gain_out, bias_out, sems):
    chan = params.shape[1]
    rows = MEL_ROWS
    wide = x3.shape[1]
    frame_dev = wide - RIM
    usable, behind, ahead = (masks[n : n + 1] for n in range(3))
    total = masks[3:4, 0:1]
    gain = params[0:1]
    count = recv.shape[0] // 14
    share = half_share(count, 9 * chan)
    sums = summed_blocks(recv, count)[0:5]
    ten = jnp.concatenate([sums[:, :chan], sums[:, chan:]], axis=0)
    bias_sum = ten[9:10]
    mean_l, inv_l = stats[chan : chan + 1, :chan], stats[chan + 8 : chan + 9, :chan]
    ten = ten - features[1:2, 0:1] * bias_sum
    k = k1t[0:9]
    gain_sum = inv_l * (jnp.sum(k * ten[0:9], axis=0, keepdims=True) - mean_l * bias_sum)
    gain_out[...] = gain_sum
    bias_out[...] = bias_sum
    factor_l = gain * inv_l
    scale = factor_l * gain_sum / total * inv_l
    scale = jnp.concatenate(
        [scale * row_valid(-1, rows)] + [scale] * rows + [scale * row_valid(rows, rows)], axis=1
    )
    many = 3 * rows

    def in_parts(v, right):
        high = lax.reduce_precision(v, 8, 7)
        v = dot(jnp.concatenate([high, v - high], axis=0).astype(BF16), right)
        return v[:many] + v[many:]

    combined = in_parts(ws[...].astype(F32) * scale, w1[2 * chan : (rows + 4) * chan, :])
    left = [recv[pl.ds(5 + p, count, stride=14), :] for p in range(share)]
    taps = TAPS // 2
    whole = [jnp.concatenate([v[:, h * chan : (h + 1) * chan] for v in left], axis=0)[:taps] for h in range(2)]
    whole = jnp.concatenate(whole, axis=0)
    for t in range(9):
        kernel_two[t] = whole[t * chan : (t + 1) * chan].T
    stores = [pltpu.make_async_copy(kernel_two, kernel_two_hbm, sems.at[4])]
    stores[0].start()
    taken = in_parts(combined, x3[...])
    taps = first[...] - taken
    moved = [taps[rows * b : rows * (b + 1)] for b in range(3)]
    mean_full = mean_l + features[1:2, 0:1] * jnp.sum(k, axis=0, keepdims=True)
    constant = jnp.sum(k * (factor_l * (bias_sum - gain_sum * inv_l * mean_full) / total), axis=1, keepdims=True)
    for a in range(3):
        row = iota((rows, 1), 0) + (a - 1) + lax.axis_index("mel") * rows
        valid = ((row >= 0) & (row < lax.axis_size("mel") * rows)).astype(F32) * usable
        for b in range(3):
            t = 3 * (2 - a) + 2 - b
            moved[b] = moved[b] - constant[t : t + 1] * valid
    result = pltpu.roll(moved[0], 1, 1) * behind + moved[1] + pltpu.roll(moved[2], wide - 1, 1) * ahead
    spec_grad[0] = (result * usable)[:, :frame_dev]
    grad_taps = factor_l * (ten[0:9] - (bias_sum * normed_taps[16:25] + gain_sum * normed_taps[0:9]) / total)
    for i in range(3):
        kernel_one[i] = grad_taps[3 * i : 3 * i + 3]
    outs = ((spec_grad, spec_hbm), (kernel_one, kernel_one_hbm), (gain_out, gain_hbm), (bias_out, bias_hbm))
    wait_all(stores + start_all(*outs, sems=sems))


def run(kernel, outs, scratch, *args, hbm=0, apart=(), flops=10**8, size=4 * 10**6):
    vmem = pl.BlockSpec(memory_space=pltpu.VMEM)
    devices = lax.axis_size("mel") * lax.axis_size("tm")
    specs = []
    args = list(args)
    for n, a in enumerate(args):
        if hbm and n >= len(args) - hbm:
            specs.append(pl.BlockSpec(memory_space=pltpu.HBM))
            args[n] = pltpu.with_memory_space_constraint(a, pltpu.HBM)
        else:
            specs.append(vmem)
            args[n] = pltpu.with_memory_space_constraint(a, pltpu.VMEM)
    return pl.pallas_call(
        kernel,
        out_shape=outs,
        in_specs=specs,
        out_specs=[pl.BlockSpec(memory_space=pltpu.HBM) if n in apart else vmem for n in range(len(outs))],
        scratch_shapes=scratch,
        compiler_params=pltpu.CompilerParams(vmem_limit_bytes=(29 + devices // 32) * 2**20),
        cost_estimate=pl.CostEstimate(flops=flops, bytes_accessed=size, transcendentals=0),
    )(*args)


def shape(dims, dtype=F32):
    return jax.ShapeDtypeStruct(dims, dtype)


def kept(dims, dtype=F32):
    return pltpu.VMEM(dims, dtype)


def far(dims, dtype=F32):
    return pltpu.HBM(dims, dtype)


def exchange(blocks, axes=AXES):
    return lax.all_to_all(blocks, axes, 0, 0, tiled=True)


def exchange_rows(rows, axes=AXES):
    return exchange(rows[:, None, :], axes)[:, 0, :]


def shards(spectrum, clip_bounds, kernel_one, gain_one, bias_one, kernel_two, gain_two, bias_two, pooled_grad):
    _, rows, frame_dev = spectrum.shape
    chan = kernel_two.shape[0]
    n_mel, n_tm = lax.axis_size("mel"), lax.axis_size("tm")
    devices = n_mel * n_tm
    half = frame_dev // 2
    wide = frame_dev + RIM
    mels = n_mel * rows

    packed, own, spec, masks = run(
        pack,
        [
            kept((devices, FIRST, 128), BF16),
            kept(pooled_grad.shape, BF16),
            kept(spectrum.shape, BF16),
            kept((8, wide)),
        ],
        [
            pltpu.SMEM(clip_bounds.shape, jnp.int32),
            pltpu.VMEM((2 * chan, half), F32),
            pltpu.VMEM((devices * FIRST, 128), F32),
            pltpu.SemaphoreType.DMA((3,)),
        ],
        spectrum,
        pooled_grad,
        clip_bounds,
        hbm=3,
    )
    recv = exchange(packed)
    ext = rows + 6
    span = 4 * 3 * chan
    wf, wb, w1, ws, pairs, singles, k1t, params, all_masks, edge_masks, twice, own_rows = run(
        weights,
        [
            kept((2 * chan, span), BF16),
            kept((2 * chan, span), BF16),
            kept((ext * chan, 128), BF16),
            far((rows * 3, (rows + 2) * chan), BF16),
            kept((chan, 128)),
            kept((chan, 128)),
            kept((16, chan)),
            kept((8, chan)),
            kept((3 * n_tm, frame_dev)),
            kept((n_tm * 8, 128)),
            kept((128, 128)),
            kept((chan * rows // 2, half), BF16),
        ],
        [
            pltpu.VMEM((9, chan, chan), BF16),
            pltpu.VMEM((3, 3, chan), BF16),
            pltpu.VMEM((4, 1, chan), F32),
            pltpu.SMEM(clip_bounds.shape, jnp.int32),
            pltpu.VMEM((rows * 3, (rows + 2) * chan), BF16),
            pltpu.VMEM((chan * rows // 2, half), F32),
            pltpu.SemaphoreType.DMA((8,)),
        ],
        own,
        clip_bounds,
        jnp.transpose(kernel_two, (2, 3, 0, 1)).reshape(9, chan, chan),
        jnp.transpose(kernel_one, (1, 2, 0)),
        gain_one[None],
        bias_one[None],
        gain_two[None],
        bias_two[None],
        hbm=7,
        apart=(3,),
    )
    pre_two, payload, act, x3, far_rim, stats_one, features = run(
        forward_one,
        [
            kept((rows * chan, wide)),
            kept((devices, SECOND, 128), BF16),
            kept((ext * 3 * chan, wide), BF16),
            kept((128, wide), BF16),
            kept((BAND, RIM)),
            kept((2 * chan + 16, 128)),
            kept((8, 128)),
        ],
        [
            pltpu.VMEM((ext * chan, wide), F32),
            pltpu.VMEM((devices * FIRST, 128), F32),
            pltpu.VMEM((n_tm * 8, 128), F32),
            pltpu.VMEM((mels + 8, RIM), F32),
            pltpu.VMEM((devices * SECOND, 128), F32),
        ],
        recv,
        spec,
        pairs,
        singles,
        twice,
        w1,
        wf,
        params,
        masks,
        all_masks,
        edge_masks,
    )
    recv = exchange(payload)
    grad, kept_half, sent_half, totals, stats_two = run(
        backward_scaled,
        [
            kept((rows * chan, frame_dev)),
            kept((TAPS // 2 + devices, 128)),
            kept((TAPS // 2 + devices, 128)),
            kept((8, 128)),
            kept((chan + 8, 128)),
        ],
        [
            pltpu.VMEM((rows // 2 * chan, frame_dev), F32),
            pltpu.VMEM((3 * chan + 16, rows * frame_dev), BF16),
            pltpu.VMEM((devices * SECOND, 128), F32),
            pltpu.VMEM((2, TAPS // 2 + devices, 128), F32),
        ],
        recv,
        pre_two,
        act,
        own_rows,
        params,
        masks,
    )
    received = lax.ppermute(sent_half, "tm", [(i, i ^ 1) for i in range(n_tm)])
    pre_ring, ring, rim, row_pairs = run(
        around,
        [kept((4 * chan, wide)), kept((4 * chan, wide)), kept((rows * chan, RIM)), kept((rows // 2 * chan, frame_dev))],
        [
            pltpu.VMEM(((rows // 2 + 2) * chan, RIM), F32),
            pltpu.VMEM((2 * chan, frame_dev), F32),
            pltpu.VMEM((devices * SECOND, 128), F32),
            pltpu.VMEM((2 * chan, half), F32),
            pltpu.VMEM((4 * 3 * chan, wide), BF16),
        ],
        recv,
        pre_two,
        act,
        w1,
        wf,
        x3,
        far_rim,
        stats_one,
        masks,
        stats_two,
    )
    (payload,) = run(
        pack_sums,
        [kept((devices * (half_share(devices, 9 * chan) + 2), 128))],
        [],
        kept_half,
        received,
        totals,
        rim,
    )
    recv = exchange_rows(payload)
    grad, own_low, payload, totals = run(
        backward,
        [
            kept(((rows + 4) * chan, wide), BF16),
            kept((rows * chan, frame_dev), BF16),
            kept((devices * 14, 128)),
            kept((8, 128)),
        ],
        [
            pltpu.VMEM(((rows + 2) * 3 * chan, frame_dev), BF16),
            pltpu.VMEM((rows * chan, frame_dev), F32),
            pltpu.VMEM((rows * chan, frame_dev), F32),
        ],
        recv,
        pre_two,
        pre_ring,
        grad,
        ring,
        rim,
        stats_two,
        w1,
        x3,
        stats_one,
        params,
        masks,
        wb,
    )
    recv = exchange_rows(payload)
    pooled, gain_two_grad, bias_two_grad = run(
        pool,
        [shape((1, chan, rows // 2, half), BF16), shape((1, chan)), shape((1, chan))],
        [
            pltpu.VMEM((rows // 2 * chan, 128), F32),
        ],
        totals,
        row_pairs,
    )
    first, ws, normed_taps = run(
        transposed,
        [
            kept((rows * 3, wide)),
            kept((rows * 3, (rows + 2) * chan), BF16),
            kept((32, chan)),
        ],
        [
            pltpu.VMEM(((rows + 2) * chan, wide), BF16),
            pltpu.VMEM((8 * 3 * chan, frame_dev), BF16),
            pltpu.VMEM(((rows + 4) * 3 * chan, RIM), BF16),
            pltpu.SemaphoreType.DMA,
        ],
        grad,
        own_low,
        w1,
        wb,
        x3,
        stats_one,
        features,
        k1t,
        params,
        masks,
        ws,
        hbm=1,
    )
    spec_grad, kernel_one_grad, kernel_two_grad, gain_one_grad, bias_one_grad = run(
        finish,
        [
            shape((1, rows, frame_dev)),
            shape((3, 3, chan)),
            shape((9, chan, chan)),
            shape((1, chan)),
            shape((1, chan)),
        ],
        [
            pltpu.VMEM((1, rows, frame_dev), F32),
            pltpu.VMEM((3, 3, chan), F32),
            pltpu.VMEM((9, chan, chan), F32),
            pltpu.VMEM((1, chan), F32),
            pltpu.VMEM((1, chan), F32),
            pltpu.SemaphoreType.DMA((5,)),
        ],
        recv,
        features,
        stats_one,
        k1t,
        first,
        ws,
        w1,
        x3,
        normed_taps,
        params,
        masks,
        apart=range(5),
    )
    kernel_two_grad = jnp.transpose(kernel_two_grad.reshape(3, 3, chan, chan), (2, 3, 0, 1))
    return (
        pooled,
        spec_grad,
        jnp.transpose(kernel_one_grad, (2, 0, 1)),
        gain_one_grad[0],
        bias_one_grad[0],
        kernel_two_grad,
        gain_two_grad[0],
        bias_two_grad[0],
    )


def solution(mesh):
    return jax.shard_map(
        shards,
        mesh=mesh,
        in_specs=(
            P(None, "mel", "tm"),
            P(),
            P(),
            P(),
            P(),
            P(),
            P(),
            P(),
            P(None, None, "mel", "tm"),
        ),
        out_specs=(P(None, None, "mel", "tm"), P(None, "mel", "tm"), P(), P(), P(), P(), P(), P()),
        check_vma=False,
    )
```

```python
import math

import jax
import jax.numpy as jnp
from jax import lax
from jax.experimental import pallas as pl
from jax.experimental.pallas import tpu as pltpu
from jax.sharding import PartitionSpec as P

F32 = jnp.float32
BF16 = jnp.bfloat16
AXES = ("mel", "tm")
EXACT = lax.Precision.HIGHEST
RIM = 128
BAND = 24
MEL_ROWS = 16
FIRST = 16
SUMS, EDGES, COLUMNS = 8, 11, 15
SIDE, FAR = 96, 112
FAR_HOLDERS = 32
TAPS = 576
SECOND = 8


def iota(shape, dim):
    return lax.broadcasted_iota(jnp.int32, shape, dim)


def dot(a, b, over=((1,), (0,)), precision=None):
    return lax.dot_general(a, b, (over, ((), ())), precision=precision, preferred_element_type=F32)


def to_column(lanes, count, start=0):
    shape = (count, lanes.shape[1])
    return jnp.sum(jnp.where(iota(shape, 1) == iota(shape, 0) + start, lanes, 0.0), axis=1, keepdims=True)


def to_lanes(column, start=0, width=128):
    shape = (column.shape[0], width)
    return jnp.sum(jnp.where(iota(shape, 1) == iota(shape, 0) + start, column, 0.0), axis=0, keepdims=True)


def halves(v):
    total = v[:, :128]
    for n in range(128, v.shape[1], 128):
        total = total + v[:, n : n + 128]
    return total


def frame_masks(bounds, frames):
    last = bounds.shape[1] - 1

    def living(f):
        return (f >= 0) & (f < bounds[0, last])

    def paired(f):
        both = living(f) & living(f + 1)
        for k in range(1, last):
            both = both & (f + 1 != bounds[0, k])
        return both

    return tuple(m.astype(F32) for m in (living(frames), paired(frames - 1), paired(frames)))


def row_valid(row, rows):
    mel = lax.axis_index("mel") * rows + row
    return ((mel >= 0) & (mel < lax.axis_size("mel") * rows)).astype(F32)


def start_all(*pairs, sems):
    copies = [pltpu.make_async_copy(src, dst, sems.at[n]) for n, (src, dst) in enumerate(pairs)]
    for copy in copies:
        copy.start()
    return copies


def wait_all(copies):
    for copy in copies:
        copy.wait()


def shifted_frames(value, behind, ahead):
    wide = value.shape[1]
    return pltpu.roll(value, 1, 1) * behind, pltpu.roll(value, wide - 1, 1) * ahead


def three_parts(v):
    high = lax.reduce_precision(v, 8, 7)
    mid = lax.reduce_precision(v - high, 8, 7)
    return high, mid, v - high - mid


def share_of(devices, chan):
    return -(-chan // devices)


def pack(spec_hbm, grad_hbm, bounds_hbm, out, own, spec, masks, bounds, edges, rows_out, sems):
    copies = start_all((spec_hbm, spec), (bounds_hbm, bounds), (grad_hbm, own), sems=sems)
    copies[1].wait()
    wide = masks.shape[1]
    frame_dev = wide - RIM
    devices = out.shape[0]
    rows = MEL_ROWS
    lane = iota((1, wide), 1)
    frames = lax.axis_index("tm") * frame_dev + jnp.where(lane < frame_dev + RIM // 2, lane, lane - wide)
    last = bounds.shape[1] - 1
    pixels = (bounds[0, last] * (lax.axis_size("mel") * rows)).astype(F32)
    found = frame_masks(bounds, frames)
    masks[...] = jnp.concatenate(
        list(found) + [jnp.full((1, wide), 1.0) * pixels, jnp.zeros((4, wide), F32)], axis=0
    )
    usable, behind, ahead = (m[:, :frame_dev] for m in found)
    copies[0].wait()
    x = spec[0].astype(F32) * usable
    lane = iota((1, frame_dev), 1)
    row = iota((rows, 1), 0)
    inner = jnp.where((lane > 0) & (lane < frame_dev - 1), usable, 0.0)
    number = (rows - 2) * jnp.sum(inner, axis=1, keepdims=True)
    inner = inner * ((row > 0) & (row < rows - 1)).astype(F32)
    centre = jnp.sum(jnp.sum(x, axis=0, keepdims=True), axis=1, keepdims=True)
    centre = centre / (rows * jnp.maximum(jnp.sum(usable, axis=1, keepdims=True), 1.0))
    centre = lax.reduce_precision(centre, 8, 7)
    shifted = [pltpu.roll(x, 1, 1) * behind, x, pltpu.roll(x, frame_dev - 1, 1) * ahead]
    taps = [pltpu.roll(v, (1 - i) % rows, 0) if i != 1 else v for i in range(3) for v in shifted]
    features = feature_rows(centre, (taps, inner))
    lane = iota((1, 128), 1)
    features = jnp.where(lane == 90, centre, jnp.where(lane == 91, number, features))
    pick = iota((8, frame_dev), 0)
    column = jnp.where(pick < 4, pick, frame_dev - 8 + pick)
    strip = dot((iota((8, frame_dev), 1) == column).astype(BF16), x.astype(BF16), ((1,), (1,)))
    lane = iota((8, 128), 1)
    repeat = (iota((rows, 128), 1) % rows == iota((rows, 128), 0)).astype(BF16)
    strip = jnp.where(lane // rows == iota((8, 128), 0), dot(strip.astype(BF16), repeat), 0.0)
    strip = jnp.sum(strip, axis=0, keepdims=True)

    def put(n, value):
        rows_out[pl.ds(n, devices, stride=FIRST), :] = jnp.broadcast_to(value, (devices, 128))

    near = jnp.concatenate([x[0:2], x[rows - 2 :]], axis=0)
    near = jnp.concatenate([near[:, :128], near[:, 128:]], axis=0)
    for d in range(devices):
        rows_out[FIRST * d : FIRST * d + 8, :] = near
    put(COLUMNS, strip)
    copies[2].wait()
    _, chan, many, half = own.shape
    share = share_of(devices, chan)
    holders = chan // share
    g = own[0].astype(F32)
    edges[0:chan] = g[:, 0, :]
    edges[chan:] = g[:, many - 1, :]

    def spread_out(v, held):
        if held < devices:
            v = jnp.concatenate([v, jnp.zeros((devices - held, 128), F32)], axis=0)
        return v

    for n in range(share):
        put(EDGES + n, spread_out(edges[n * holders : (n + 1) * holders, :], holders))
        put(EDGES + share + n, spread_out(edges[chan + n * holders : chan + (n + 1) * holders, :], holders))
    for n in range(2 * share, COLUMNS - EDGES):
        put(EDGES + n, jnp.zeros((1, 128), F32))
    end = iota((8, half), 0)
    at = iota((8, half), 1)
    ends = ((end == 0) & (at == 0)) | ((end == 1) & (at == half - 1))
    columns = dot(ends.astype(BF16), g.reshape(chan * many, half).astype(BF16), ((1,), (1,)))
    group = 128 // many
    source = iota((128, 128), 0)
    lane = iota((group, 128), 1)
    mine = lane // many == iota((group, 128), 0)
    lane8, own8 = iota((8, 128), 1), iota((8, 128), 0)
    parts = three_parts(features)
    for n in range(2):
        side = jnp.zeros((holders, 128), F32)
        for m in range(share):
            move = (iota((128, 128), 1) == SIDE + many * m + source % many).astype(BF16)
            first = m * holders * many // 128
            block = [columns[n : n + 1, 128 * q : 128 * (q + 1)] for q in range(first, first + holders * many // 128)]
            block = jnp.concatenate([jnp.where(mine, v, 0.0) for v in block], axis=0)
            side = side + dot(block.astype(BF16), move)
        far = x[2:4] if n == 0 else x[rows - 4 : rows - 2]
        pieces = [far[r : r + 1, 128 * h : 128 * (h + 1)] for r in range(2) for h in range(2)]
        pieces = jnp.concatenate([jnp.where(lane8 // 16 == own8, v, 0.0) for v in pieces], axis=0)
        far = dot(pieces.astype(BF16), (iota((128, 128), 1) == FAR + source % 16).astype(BF16))
        put(SUMS + n, spread_out(side, holders) + spread_out(far, FAR_HOLDERS) + parts[n])
    put(SUMS + 2, parts[2])
    out[...] = rows_out[...].reshape(out.shape).astype(BF16)


def weights(own, bounds_hbm, k2_hbm, k1_hbm, gain_one_hbm, bias_one_hbm, gain_two_hbm, bias_two_hbm,
            wf, wb, w1, ws_hbm, pairs, singles, k1t, params, all_masks, edge_masks, twice, own_rows,
            k2, k1, vectors, bounds, ws, temp, sems):
    loads = start_all(
        (bounds_hbm, bounds),
        (k2_hbm, k2),
        (k1_hbm, k1),
        (gain_one_hbm, vectors.at[0]),
        (bias_one_hbm, vectors.at[1]),
        (gain_two_hbm, vectors.at[2]),
        (bias_two_hbm, vectors.at[3]),
        sems=sems,
    )
    _, many, count, half = own.shape
    temp[...] = own[0].astype(F32).reshape(many * count, half)
    for r in range(count):
        own_rows[r * many : (r + 1) * many] = temp[pl.ds(r, many, stride=count), :].astype(BF16)
    wait_all(loads)
    chan = k2.shape[1]
    span = wf.shape[1]
    taps = [k2[t].astype(F32) for t in range(9)]
    rest = jnp.zeros((chan, span - 9 * chan), F32)
    forward = jnp.concatenate(taps + [rest], axis=1)
    backward = jnp.concatenate([taps[8 - t].T for t in range(9)] + [rest], axis=1)
    for r in range(wb.shape[0] // chan):
        at = slice(r * chan, (r + 1) * chan)
        wb[at] = (pltpu.roll(backward, 3 * chan * r, 1) if r else backward).astype(BF16)
    full = jnp.concatenate([k1[n].astype(F32) for n in range(3)] + [jnp.zeros((7, chan), F32)], axis=0)
    low = [
        jnp.concatenate([full[3 * (2 - a) + 2 - b : 3 * (2 - a) + 3 - b] for a in range(3)], axis=1)
        for b in range(3)
    ]
    rest = jnp.zeros((1, ws.shape[1] - 3 * chan), F32)
    for b in range(3):
        base = jnp.concatenate([low[b], rest], axis=1)
        many = ws.shape[0] // 3
        rolled = [pltpu.roll(base, chan * m, 1) if m else base for m in range(many)]
        ws[many * b : many * (b + 1)] = jnp.concatenate(rolled, axis=0).astype(BF16)
    store_ws = pltpu.make_async_copy(ws, ws_hbm, sems.at[7])
    store_ws.start()
    count, frame_dev = all_masks.shape[0] // 3, all_masks.shape[1]
    frames = iota((count, frame_dev), 0) * frame_dev + iota((count, frame_dev), 1)
    for n, mask in enumerate(frame_masks(bounds, frames)):
        all_masks[n * count : (n + 1) * count] = mask
    q = iota(edge_masks.shape, 0)
    lane = iota(edge_masks.shape, 1)
    k = q % 8
    frames = (q // 8) * frame_dev + jnp.where(k < 4, k, k + frame_dev - 8)
    living, behind, ahead = frame_masks(bounds, frames)
    living = jnp.where((k == 0) | (k == 7), living, 0.0)
    edge_masks[...] = jnp.where(lane == 0, living, jnp.where(lane == 1, behind, jnp.where(lane == 2, ahead, 0.0)))
    params[...] = jnp.concatenate(
        [vectors[n] for n in range(4)] + [jnp.zeros((4, chan), F32)], axis=0
    )
    tap = iota((16, 128), 0)
    lane = iota((16, 128), 1)
    i = (tap * 11) >> 5
    ninth = (lane * 57) >> 9
    to_band = (lane == BAND * (tap - 3 * i) + i) & (tap < 9)
    to_left = (ninth == tap) & (tap < 9)
    to_right = (lane - 9 * ninth == tap) & (lane < 81)
    to_single = (lane == 81 + tap) & (tap < 9)
    source = iota((128, 128), 0) - 81
    lane = iota((128, 128), 1)
    ninth = (lane * 57) >> 9
    inside = (source >= 0) & (source < 9) & (lane < 81)
    twice[...] = jnp.where(inside, (source == ninth).astype(F32) + (source == lane - 9 * ninth).astype(F32), 0.0)
    for r in range(wf.shape[0] // chan):
        at = slice(r * chan, (r + 1) * chan)
        wf[at] = (pltpu.roll(forward, 3 * chan * r, 1) if r else forward).astype(BF16)
    k1t[...] = full
    k = full.astype(BF16)
    lanes = [dot(k, select.astype(BF16), ((0,), (0,))) for select in (to_band, to_left, to_right, to_single)]
    pairs[...] = lanes[1] * lanes[2]
    singles[...] = lanes[3]
    for m in range(w1.shape[0] // chan):
        w1[m * chan : (m + 1) * chan] = (pltpu.roll(lanes[0], m, 1) if m else lanes[0]).astype(BF16)
    store_ws.wait()


def feature_rows(centre, *parts):
    def folded(v):
        return jnp.sum(halves(v), axis=0, keepdims=True)

    rows = [jnp.zeros((1, 128), F32)] * 96
    for taps, weight in parts:
        z = [tap - centre for tap in taps]
        for s in range(9):
            left = z[s] * weight
            rows[81 + s] = rows[81 + s] + folded(left)
            for t in range(s, 9):
                rows[9 * s + t] = rows[9 * t + s] = rows[9 * s + t] + folded(left * z[t])
    return to_lanes(jnp.sum(jnp.concatenate(rows, axis=0), axis=1, keepdims=True))


def summed_blocks(ref, devices, by=1):
    block = ref.shape[0] // devices
    period = max(8 // math.gcd(block, 8), by)
    step = period * block
    total = ref[0:step, :]
    for at in range(step, ref.shape[0], step):
        total = total + ref[at : at + step, :]
    results = []
    for first in range(by):
        result = total[first * block : (first + 1) * block]
        for n in range(first + by, period, by):
            result = result + total[n * block : (n + 1) * block]
        results.append(result)
    return results if by > 1 else results[0]


def moved_rows(v, step):
    if step == 0:
        return v
    count = v.shape[0]
    if abs(step) >= count:
        return jnp.zeros_like(v)
    zero = jnp.zeros((abs(step), v.shape[1]), v.dtype)
    if step > 0:
        return jnp.concatenate([zero, v[: count - step]], axis=0)
    return jnp.concatenate([v[-step:], zero], axis=0)


def silu_halves(h):
    t = jnp.tanh(h)
    one = 1.0 + t
    return h * one, one * (1.0 + h * (1.0 - t))


def act_row(act, r, low, low_masks):
    low = low * low_masks[0]
    chan = low.shape[0]
    for n, v in enumerate((low,) + shifted_frames(low, *low_masks[1:])):
        at = (3 * r + (1, 0, 2)[n]) * chan
        act[at : at + chan, :] = v


def forward_one(recv, spec, pairs, singles, twice, w1, wf, params, masks, all_masks, edge_masks,
                pre_two, payload, act, x3, far_rim, stats, features_out, pre_one, got, strips, halo, rows_out):
    devices = recv.shape[0]
    n_mel, count = lax.axis_size("mel"), lax.axis_size("tm")
    rows = MEL_ROWS
    mels = n_mel * rows
    wide = masks.shape[1]
    frame_dev = wide - RIM
    chan = params.shape[1]
    me_m, me_t = lax.axis_index("mel"), lax.axis_index("tm")
    usable, behind, ahead = (masks[n : n + 1] for n in range(3))
    total = masks[3:4, 0:1]
    got[...] = recv[...].astype(F32).reshape(devices * FIRST, 128)

    def every(n):
        return got[pl.ds(n, devices, stride=FIRST), :]

    lane = iota((count, 128), 1)
    bands = [got[pl.ds(FIRST * k * count + COLUMNS, count, stride=FIRST), :] for k in range(n_mel)]
    for c in range(8):
        column = jnp.zeros((count, 128), F32)
        for k, band in enumerate(bands):
            part = jnp.where(lane // rows == c, band, 0.0)
            column = column + (pltpu.roll(part, rows * (k - c) % 128, 1) if k != c else part)
        strips[pl.ds(c, count, stride=8), :] = column
    at = pl.multiple_of(FIRST * (jnp.maximum(me_m - 1, 0) * count + me_t), 8)
    above = got[pl.ds(at, 8), :] * (me_m > 0).astype(F32)
    at = pl.multiple_of(FIRST * (jnp.minimum(me_m + 1, n_mel - 1) * count + me_t), 8)
    below = got[pl.ds(at, 8), :] * (me_m < n_mel - 1).astype(F32)
    above = jnp.concatenate([above[2:4], above[6:8]], axis=1)
    below = jnp.concatenate([below[0:2], below[4:6]], axis=1)
    own = spec[0].astype(F32) * usable[:, :frame_dev]
    at = pl.multiple_of(8 * jnp.minimum(me_t + 1, count - 1), 8)
    after = strips[pl.ds(at, 8), :][:, :mels] * (me_t + 1 < count).astype(F32)
    at = pl.multiple_of(8 * jnp.maximum(me_t - 1, 0), 8)
    before = strips[pl.ds(at, 8), :][:, :mels] * (me_t > 0).astype(F32)
    sides = jnp.concatenate([after[0:4], before[4:8], jnp.zeros((8, mels), F32)], axis=0).astype(BF16)
    side = iota((16, RIM), 0)
    place = iota((16, RIM), 1) == jnp.where(side < 4, side, jnp.where(side < 8, side + RIM - 8, -1))
    halo[0:8] = jnp.zeros((8, RIM), F32)
    halo[mels : mels + 8] = jnp.zeros((8, RIM), F32)
    halo[4 : mels + 4] = dot(sides, place.astype(BF16), ((0,), (0,)))
    rim = halo[pl.ds(pl.multiple_of(me_m * rows, 8), BAND), :]
    far_rim[...] = rim
    row = iota((BAND, RIM), 0)
    rim = jnp.where((row >= 2) & (row < BAND - 2), rim, 0.0)
    blank = jnp.zeros((2, frame_dev), F32)
    near = jnp.concatenate([jnp.concatenate([blank, above, own, below, blank], axis=0), rim], axis=1)
    x3[...] = jnp.concatenate(
        [
            pltpu.roll(near, 1, 1) * behind,
            near,
            pltpu.roll(near, wide - 1, 1) * ahead,
            jnp.broadcast_to(usable, (BAND, wide)),
            jnp.zeros((128 - 4 * BAND, wide), F32),
        ],
        axis=0,
    ).astype(BF16)
    pre_one[2 * chan : (rows + 4) * chan] = dot(w1[2 * chan : (rows + 4) * chan, :], x3[...])
    lane = iota((1, 128), 1)
    parts = jnp.where(lane < 92, every(SUMS) + every(SUMS + 1) + every(SUMS + 2), 0.0)
    centres, numbers = parts[:, 90:91], parts[:, 91:92]
    centre = jnp.sum(centres * numbers, axis=0, keepdims=True)
    centre = centre / jnp.maximum(jnp.sum(numbers, axis=0, keepdims=True), 1.0)
    delta = centres - centre
    features = jnp.sum(parts + delta * numbers * jnp.where(lane < 81, delta, 1.0), axis=0, keepdims=True)
    moved = jnp.sum(delta * parts, axis=0, keepdims=True)
    def edge_row(k, n):
        first = FIRST * k * count + n
        return jnp.concatenate(
            [got[pl.ds(first, count, stride=FIRST), :], got[pl.ds(first + 4, count, stride=FIRST), :]], axis=1
        )

    edge_rows = [[edge_row(k, n) for n in range(4)] for k in range(n_mel)]
    zero = jnp.zeros((count, frame_dev), F32)
    rows_of = [[], [], []]
    for k, (top, second, fore, bottom) in enumerate(edge_rows):
        for n, v in enumerate((edge_rows[k - 1][3] if k else zero, top, second)):
            rows_of[n].append(v)
        for n, v in enumerate((fore, bottom, edge_rows[k + 1][0] if k + 1 < n_mel else zero)):
            rows_of[n].append(v)
    f_usable, f_behind, f_ahead = (all_masks[n * count : (n + 1) * count, :] for n in range(3))
    lane = iota((count, frame_dev), 1)

    def frame_before(v):
        v = pltpu.roll(v, 1, 1)
        return jnp.where(lane == 0, pltpu.roll(v, 1, 0), v) * f_behind

    def frame_after(v):
        v = pltpu.roll(v, frame_dev - 1, 1)
        return jnp.where(lane == frame_dev - 1, pltpu.roll(v, count - 1, 0), v) * f_ahead

    taps = []
    for group in rows_of:
        for move in (frame_before, lambda v: v, frame_after):
            taps.append(jnp.concatenate([move(v) for v in group], axis=1))
    f_usable = jnp.concatenate([f_usable] * (2 * n_mel), axis=1)
    borders = (taps, f_usable)
    edge = strips[...]
    q_usable, q_behind, q_ahead = (edge_masks[:, n : n + 1] for n in range(3))
    lane = iota((count * 8, 128), 1)
    inside = (lane < mels) & (lane % rows != 0) & (lane % rows != rows - 1)
    shifted = [
        pltpu.roll(edge, 1, 0) * q_behind,
        edge,
        pltpu.roll(edge, count * 8 - 1, 0) * q_ahead,
    ]
    taps = [pltpu.roll(v, (1 - i) % 128, 1) if i != 1 else v for i in range(3) for v in shifted]
    features = features + feature_rows(centre, borders, (taps, jnp.where(inside, q_usable, 0.0)))
    features = jnp.where(iota((1, 128), 1) < 90, features, 0.0)
    near_mean = jnp.sum(singles[...] * features, axis=1, keepdims=True) / total
    around = jnp.sum(singles[...], axis=1, keepdims=True)
    square = jnp.sum(pairs[...] * features, axis=1, keepdims=True)
    square = (square + 2.0 * around * jnp.sum(singles[...] * moved, axis=1, keepdims=True)) / total
    inv = lax.rsqrt(square - near_mean * near_mean + 1e-05)
    mean = near_mean + centre * around
    lane = iota((chan, 128), 1)
    stats[0:chan] = jnp.where(lane == 0, mean, jnp.where(lane == 1, inv, 0.0))
    stats[chan : chan + 8] = jnp.broadcast_to(to_lanes(near_mean), (8, 128))
    stats[chan + 8 : chan + 16] = jnp.broadcast_to(to_lanes(inv), (8, 128))
    scale = 0.5 * to_column(params[0:1], chan) * inv
    shift = 0.5 * to_column(params[1:2], chan) - mean * scale
    stats[chan + 16 :] = jnp.where(lane == 0, scale, jnp.where(lane == 1, shift, 0.0))
    scale = jnp.broadcast_to(scale, (chan, wide))
    shift = jnp.broadcast_to(shift, (chan, wide))
    block, taps = wf.shape
    first = jnp.zeros((chan, 128), F32)
    second = jnp.zeros((chan, 128), F32)
    own_mask = usable[:, :frame_dev]
    low_masks = [m.astype(BF16) for m in (usable, behind, ahead)]
    for r in range(2, rows + 4):
        value, _ = silu_halves(pre_one[r * chan : (r + 1) * chan, :] * scale + shift)
        if not 0 <= r - 3 < rows:
            value = value * row_valid(r - 3, rows)
        act_row(act, r, value.astype(BF16), low_masks)
        if r < 5 or r % 2 == 0:
            continue
        g = (r - 3) // 2
        result = dot(wf[...], act[g * 3 * block : g * 3 * block + taps, :frame_dev])
        at = (g - 1) * block
        pre_two[at : at + block, :frame_dev] = result
        if g % 2 == 0:
            beside = [act[n * 3 * block : n * 3 * block + taps, frame_dev:] for n in (g - 1, g)]
            beside = dot(wf[...], jnp.concatenate(beside, axis=1))
            for n in range(2):
                pre_two[at + (n - 1) * block : at + n * block, frame_dev:] = beside[:, n * RIM : (n + 1) * RIM]
        for q in range(2):
            p = result[q * chan : (q + 1) * chan]
            masked = p * own_mask
            first = first + halves(masked)
            second = second + halves(masked * p)
    moved = dot(jnp.broadcast_to(moved, (8, 128)), twice[...], precision=EXACT)[0:1]
    features_out[...] = jnp.concatenate(
        [features + moved, jnp.broadcast_to(centre, (1, 128)), jnp.zeros((6, 128), F32)], axis=0
    )
    share = share_of(devices, chan)

    def put(n, value):
        rows_out[pl.ds(n, devices, stride=SECOND), :] = jnp.broadcast_to(value, (devices, 128))

    for n in range(share):
        put(3 + n, moved_rows(every(EDGES + share + n), count))
        put(3 + share + n, moved_rows(every(EDGES + n), -count))
    for n in [0, 1, 2] + list(range(3 + 2 * share, SECOND - 1)):
        put(n, jnp.zeros((1, 128), F32))
    lane = iota((devices, 128), 1)
    tm = iota((devices, 128), 0) % count
    at_side = (lane >= SIDE) & (lane < FAR)
    lefts = jnp.where(at_side, every(SUMS), 0.0)
    rights = jnp.where(at_side, every(SUMS + 1), 0.0)
    beside = jnp.zeros((devices, 128), F32)
    for n, step in enumerate((0, count, -count)):
        one = jnp.where(tm > 0, moved_rows(rights, step + 1), 0.0)
        two = jnp.where(tm < count - 1, moved_rows(lefts, step - 1), 0.0)
        beside = beside + pltpu.roll(one, (32 * n - SIDE) % 128, 1) + pltpu.roll(two, (32 * n + 16 - SIDE) % 128, 1)
    outer = jnp.where(lane >= FAR, moved_rows(every(SUMS + 1), count), 0.0)
    beside = beside + pltpu.roll(outer, 128 - 16, 1)
    beside = beside + jnp.where(lane >= FAR, moved_rows(every(SUMS), -count), 0.0)
    put(SECOND - 1, beside)
    first = jnp.sum(first, axis=1, keepdims=True)
    second = jnp.sum(second, axis=1, keepdims=True)
    parts = list(three_parts(to_lanes(first) + to_lanes(second, chan)))
    parts = jnp.concatenate(parts + [jnp.zeros((SECOND - 3, 128), F32)], axis=0)
    for d in range(devices):
        payload[d] = (rows_out[SECOND * d : SECOND * (d + 1), :] + parts).astype(BF16)


def spreading(half):
    lane = iota((half, 2 * half), 1)
    return jnp.where(lane >> 1 == iota((half, 2 * half), 0), 0.25, 0.0).astype(BF16)


def half_share(devices, taps):
    return -(-taps // 2 // devices)


def backward_scaled(recv, pre_two, act, own_rows, params, masks,
                    grad, kept_half, sent_half, totals, stats, up, right, halved):
    devices = recv.shape[0]
    chan = params.shape[1]
    half = own_rows.shape[1]
    frame_dev = 2 * half
    rows = MEL_ROWS
    up[...] = dot(own_rows[...], spreading(half))
    usable = masks[0:1, :frame_dev]
    total = masks[3:4, 0:1]
    sums = [recv[d].astype(F32) for d in range(devices)]
    while len(sums) > 1:
        sums = [a + b for a, b in zip(sums[0::2], sums[1::2])]
    sums = jnp.sum(sums[0][0:3], axis=0, keepdims=True)
    mean = to_column(sums, chan) / total
    inv = lax.rsqrt(to_column(sums, chan, chan) / total - mean * mean + 1e-05)
    scale = 0.5 * to_column(params[2:3], chan) * inv
    shift = 0.5 * to_column(params[3:4], chan) - mean * scale
    lane = iota((chan, 128), 1)
    columns = jnp.zeros((chan, 128), F32)
    for n, column in enumerate((mean, inv, scale, shift)):
        columns = jnp.where(lane == n, column, columns)
    stats[0:chan] = columns
    stats[chan : chan + 8] = jnp.broadcast_to(to_lanes(inv), (8, 128))
    mean, inv, scale, shift = (jnp.broadcast_to(v, (chan, frame_dev)) for v in (mean, inv, scale, shift))
    first = jnp.zeros((chan, 128), F32)
    second = jnp.zeros((chan, 128), F32)
    mask = 0.5 * usable
    right[3 * chan :] = jnp.ones((16, rows * frame_dev), BF16)
    table = jnp.zeros((9 * chan, 3 * chan + 16), F32)
    for m in range(rows):
        at = slice(m * chan, (m + 1) * chan)
        pre = pre_two[at, :frame_dev]
        _, slope = silu_halves(pre * scale + shift)
        g = up[m // 2 * chan : (m // 2 + 1) * chan, :] * slope * mask
        grad[at, :] = g
        normed = (pre - mean) * inv
        first = first + halves(g * normed)
        second = second + halves(g)
        lanes = slice(m * frame_dev, (m + 1) * frame_dev)
        right[0:chan, lanes] = g.astype(BF16)
        right[chan : 2 * chan, lanes] = normed.astype(BF16)
        right[2 * chan : 3 * chan, lanes] = (g - right[0:chan, lanes].astype(F32)).astype(BF16)
        if m in (5, 11, rows - 1):
            start = m - m % 6
            left = [act[(n + 2) * 3 * chan : (n + 5) * 3 * chan, :frame_dev] for n in range(start, m + 1)]
            lanes = slice(start * frame_dev, (m + 1) * frame_dev)
            table = table + dot(jnp.concatenate(left, axis=1), right[:, lanes], ((1,), (1,)))
    first = jnp.sum(first, axis=1, keepdims=True)
    second = jnp.sum(second, axis=1, keepdims=True)
    totals[...] = jnp.broadcast_to(to_lanes(first) + to_lanes(second, chan), (8, 128))
    rest = jnp.concatenate([table[:, 2 * chan :], jnp.zeros((9 * chan, chan - 16), F32)], axis=1)
    both = table[:, : 2 * chan] + jnp.where(iota(rest.shape, 1) < chan, rest, 0.0)
    single = rest[:, chan : chan + 1]
    taps = 9 * chan // 2
    lane = iota((devices, 128), 1)
    for h in range(2):
        halved[h, 0:taps] = both[h * taps : (h + 1) * taps]
        constants = jnp.zeros((devices, 128), F32)
        for k in range(half_share(devices, 9 * chan)):
            at = h * taps + k * devices
            ones = single[at : min(at + devices, (h + 1) * taps)]
            if ones.shape[0] < devices:
                ones = jnp.concatenate([ones, jnp.zeros((devices - ones.shape[0], 1), F32)], axis=0)
            constants = jnp.where(lane == k, ones, constants)
        halved[h, taps:] = constants
    core = lax.axis_index("tm") % 2
    kept_half[...] = halved[core]
    sent_half[...] = halved[1 - core]


def around(recv, pre_two, act, w1, wf, x3, far_rim, stats_one, masks, stats, pre_ring, ring, rim, pairs,
           sides, up, got, beyond, more):
    devices = recv.shape[0]
    got[...] = recv[:, 0:SECOND, :].astype(F32).reshape(devices * SECOND, 128)
    rows = MEL_ROWS
    many = rows // 2
    wide = pre_two.shape[1]
    frame_dev = wide - RIM
    chan = pre_two.shape[0] // rows
    usable = masks[0:1]
    low_masks = [masks[n : n + 1].astype(BF16) for n in range(3)]
    pieces = got[pl.ds(SECOND - 1, devices, stride=SECOND), :][:FAR_HOLDERS].astype(BF16)
    source = iota((128, 128), 0)
    lane = iota((FAR_HOLDERS, 128), 1)
    mine = lane // 16 == iota((FAR_HOLDERS, 128), 0) % 8
    outer = []
    for first in (SIDE, FAR):
        place = (source - first == iota((128, 128), 1) % 16).astype(BF16)
        v = jnp.where(mine, dot(pieces, place), 0.0)
        v = [jnp.sum(v[8 * n : 8 * n + 8], axis=0, keepdims=True) for n in range(4)]
        outer += [jnp.concatenate(v[2 * r : 2 * r + 2], axis=1) for r in range(2)]
    blank = jnp.zeros((BAND - 4, frame_dev), F32)
    far = jnp.concatenate(outer[:2] + [blank] + outer[2:], axis=0)
    row = iota((BAND, RIM), 0)
    far = jnp.concatenate([far, jnp.where((row < 2) | (row >= BAND - 2), far_rim[...], 0.0)], axis=1)
    far = jnp.concatenate(
        [
            pltpu.roll(far, 1, 1) * masks[1:2],
            far,
            pltpu.roll(far, wide - 1, 1) * masks[2:3],
            jnp.zeros((128 - 3 * BAND, wide), F32),
        ],
        axis=0,
    )
    x_all = (x3[...].astype(F32) + far).astype(BF16)
    scale = jnp.broadcast_to(stats_one[chan + 16 :, 0:1], (chan, wide))
    shift = jnp.broadcast_to(stats_one[chan + 16 :, 1:2], (chan, wide))
    for h, start in enumerate((0, rows + 4)):
        pre_one = dot(w1[start * chan : (start + 2) * chan, :], x_all)
        for n in range(2):
            value, _ = silu_halves(pre_one[n * chan : (n + 1) * chan] * scale + shift)
            value = value * row_valid(start + n - 3, rows)
            act_row(more, 2 * h + n, value.astype(BF16), low_masks)
    line = 3 * chan
    above = jnp.concatenate([more[0 : 2 * line, :], act[2 * line : 4 * line, :]], axis=0)
    below = jnp.concatenate([act[(rows + 2) * line : (rows + 4) * line, :], more[2 * line :, :]], axis=0)
    pre_ring[0 : 2 * chan] = dot(wf[...], above)
    pre_ring[2 * chan :] = dot(wf[...], below)
    share = share_of(devices, chan)
    holders = chan // share

    def every(n):
        return got[pl.ds(n, devices, stride=SECOND), :]

    beside = 0.25 * every(SECOND - 1)[:holders]
    lane = iota((holders, RIM), 1)
    for n in range(share):
        first = n * holders
        beyond[first : first + holders, :] = every(3 + n)[:holders]
        beyond[chan + first : chan + first + holders, :] = every(3 + share + n)[:holders]
        for r in range(many + 2):
            at = many * n + (r if r < many else 32 + many - 1 if r == many else 64)
            left, right_of = beside[:, at : at + 1], beside[:, at + 16 : at + 17]
            side = jnp.where(lane >= RIM - 2, left, jnp.where(lane < 2, right_of, 0.0))
            sides[r * chan + first : r * chan + first + holders, :] = side
    up[...] = dot(beyond[...].astype(BF16), spreading(frame_dev // 2))
    scale = jnp.broadcast_to(stats[0:chan, 2:3], (chan, wide))
    shift = jnp.broadcast_to(stats[0:chan, 3:4], (chan, wide))
    for n, m in enumerate((-2, -1, rows, rows + 1)):
        below = n // 2
        upstream = jnp.concatenate(
            [
                up[below * chan : (below + 1) * chan, :],
                sides[(many + below) * chan : (many + below + 1) * chan, :],
            ],
            axis=1,
        )
        _, slope = silu_halves(pre_ring[n * chan : (n + 1) * chan, :] * scale + shift)
        ring[n * chan : (n + 1) * chan, :] = upstream * slope * (usable * (0.5 * row_valid(m, rows)))
    both = None
    for m in range(rows):
        at = slice(m * chan, (m + 1) * chan)
        _, slope = silu_halves(pre_two[at, frame_dev:] * scale[:, frame_dev:] + shift[:, frame_dev:])
        upstream = sides[m // 2 * chan : (m // 2 + 1) * chan, :]
        rim[m * chan : (m + 1) * chan, :] = upstream * slope * (0.5 * usable[:, frame_dev:])
        value, _ = silu_halves(pre_two[at, :frame_dev] * scale[:, :frame_dev] + shift[:, :frame_dev])
        value = value * usable[:, :frame_dev]
        both = value if m % 2 == 0 else both + value
        if m % 2:
            pairs[m // 2 * chan : (m // 2 + 1) * chan, :] = both


def pack_sums(kept_half, received, totals, after, payload):
    del after
    devices = kept_half.shape[0] - TAPS // 2
    block = payload.shape[0] // devices
    payload[pl.ds(0, devices, stride=block), :] = jnp.broadcast_to(totals[0:1], (devices, 128))
    taps = TAPS // 2
    total = kept_half[...] + received[...]
    for k in range(block - 2):
        cut = total[k * devices : min((k + 1) * devices, taps)]
        if cut.shape[0] < devices:
            cut = jnp.concatenate([cut, jnp.zeros((devices - cut.shape[0], 128), F32)], axis=0)
        payload[pl.ds(1 + k, devices, stride=block), :] = cut
    payload[pl.ds(block - 1, devices, stride=block), :] = total[taps:]


def pool(totals, pairs, out, gain_out, bias_out, temp):
    gain_out[...] = totals[0:1, : gain_out.shape[1]]
    bias_out[...] = totals[0:1, gain_out.shape[1] :]
    chan, rows, half = out.shape[1:]
    to_mean = jnp.where(iota((2 * half, half), 0) >> 1 == iota((2 * half, half), 1), 0.25, 0.0)
    pooled = dot(pairs[...], to_mean, precision=EXACT)
    for r in range(rows):
        temp[pl.ds(r, chan, stride=rows), :] = pooled[r * chan : (r + 1) * chan]
    out[0] = temp[...].reshape(chan, rows, half).astype(BF16)


def backward(recv, pre_two, pre_ring, grad, ring, rim, stats_two, w1, x3, stats, params, masks, wb,
             out, own_low, payload, totals, g3, pre_one, g1):
    chan = params.shape[1]
    rows = MEL_ROWS
    wide = pre_two.shape[1]
    frame_dev = wide - RIM
    usable = masks[0:1]
    behind, ahead = (masks[n : n + 1].astype(BF16) for n in (1, 2))
    total = masks[3:4, 0:1]
    devices = payload.shape[0] // 14
    pre_one[...] = dot(w1[3 * chan : (rows + 3) * chan], x3[:, :frame_dev])

    even, odd = summed_blocks(recv, devices, 2)
    sums = even[0:1] + odd[0:1]
    gain_sum, bias_sum = sums[:, :chan], sums[:, chan:]
    totals[...] = jnp.broadcast_to(sums, (8, 128))
    mean, inv = stats_two[0:chan, 0:1], stats_two[0:chan, 1:2]
    factor = to_column(params[2:3], chan) * inv
    gain_part = factor * (to_column(sums, chan) / total * inv)
    bias_part = factor * (to_column(sums, chan, chan) / total) - mean * gain_part
    gain_part = jnp.broadcast_to(gain_part, (chan, wide))
    bias_part = jnp.broadcast_to(bias_part, (chan, wide))
    factor = jnp.broadcast_to(factor, (chan, wide))
    scale = jnp.broadcast_to(stats[chan + 16 :, 0:1], (chan, frame_dev))
    shift = jnp.broadcast_to(stats[chan + 16 :, 1:2], (chan, frame_dev))
    factor_one = jnp.broadcast_to(to_column(params[0:1], chan) * stats[0:chan, 1:2], (chan, frame_dev))
    own_mask = 0.5 * usable[:, :frame_dev]
    count = rows + 4
    share = even.shape[0] - 2
    mine = jnp.concatenate([even[1 : share + 1], odd[1 : share + 1]], axis=0)
    single = jnp.concatenate([to_column(v[share + 1 :], share) for v in (even, odd)], axis=0)
    factor_l = params[2:3] * stats_two[chan : chan + 1, :chan]
    mine = mine[:, :chan] - (bias_sum * single + gain_sum * mine[:, chan:]) / total
    mine = factor_l * mine
    mine = jnp.concatenate([mine[:share], mine[share:]], axis=1)
    if share < 9:
        mine = jnp.concatenate([mine, jnp.zeros((9 - share, 128), F32)], axis=0)
    table = jnp.zeros((chan, 128), F32)

    def tap_sums(m):
        part = g1[m * chan : (m + 4) * chan, :]
        high = lax.reduce_precision(part, 8, 7)
        low = (part - high).astype(BF16)
        taps_in = x3[:, :frame_dev]
        products = dot(high.astype(BF16), taps_in, ((1,), (1,))) + dot(low, taps_in, ((1,), (1,)))
        moved = [pltpu.roll(products[k * chan : (k + 1) * chan], 128 - (m + k + 3), 1) for k in range(4)]
        return (moved[0] + moved[1]) + (moved[2] + moved[3])

    for q in range(count):
        at = slice(q * chan, (q + 1) * chan)
        mask = usable if 0 <= q - 2 < rows else usable * row_valid(q - 2, rows)
        if 2 <= q < rows + 2:
            own = slice((q - 2) * chan, (q - 1) * chan)
            pre, scaled = pre_two[own, :], jnp.concatenate([grad[own, :], rim[own, :]], axis=1)
        else:
            n = q if q < 2 else q - rows
            pre, scaled = pre_ring[n * chan : (n + 1) * chan, :], ring[n * chan : (n + 1) * chan, :]
        low = (factor * scaled - (bias_part + pre * gain_part) * mask).astype(BF16)
        out[at, :] = low
        if not 1 <= q < count - 1:
            continue
        base = (q - 1) * 3 * chan
        for n, v in enumerate((low,) + shifted_frames(low, behind, ahead)):
            spot = base + (1, 0, 2)[n] * chan
            g3[spot : spot + chan, :] = v[:, :frame_dev]
        start = q - 4
        if start < 0 or start % 2:
            continue
        result = dot(wb[...], g3[start * 3 * chan : (start + 4) * 3 * chan, :])
        for n in range(2):
            m = start + n
            at = slice(m * chan, (m + 1) * chan)
            _, slope = silu_halves(pre_one[at, :] * scale + shift)
            value = result[n * chan : (n + 1) * chan] * slope * own_mask
            own_low[at, :] = (value * factor_one).astype(BF16)
            g1[at, :] = value
        if start % 4 == 2 and start > 2:
            table = table + tap_sums(start - 6)
    table = table + tap_sums(rows - 4)
    table = table.T
    places = [BAND * j + i for i in range(3) for j in range(3)] + [3 * BAND]
    rows10 = jnp.concatenate([table[n : n + 1] for n in places], axis=0)
    sums = jnp.concatenate([rows10[0:5], rows10[5:10]], axis=1)
    block = jnp.concatenate([sums, mine], axis=0)
    block = jnp.concatenate([block] * 4, axis=0)
    for d in range(0, devices, 4):
        payload[14 * d : 14 * (d + 4), :] = block


def transposed(grad, own_low, w1, wb, x3, stats, features, k1t, params, masks, ws_hbm,
               first, ws, normed_taps, low, g3, rim, sem):
    load = pltpu.make_async_copy(ws_hbm, ws, sem)
    load.start()
    rows = MEL_ROWS
    chan = own_low.shape[0] // rows
    wide = grad.shape[1]
    frame_dev = wide - RIM
    count = grad.shape[0] // chan
    usable = masks[0:1]
    behind, ahead = (masks[n : n + 1].astype(BF16) for n in (1, 2))
    scale = jnp.broadcast_to(stats[chan + 16 :, 0:1], (chan, wide))
    shift = jnp.broadcast_to(stats[chan + 16 :, 1:2], (chan, wide))
    factor = jnp.broadcast_to(to_column(params[0:1], chan) * stats[0:chan, 1:2], (chan, wide))
    edge = (0, 1, 2, 3, count - 4, count - 3, count - 2, count - 1)
    for q in range(count):
        value = grad[q * chan : (q + 1) * chan, :]
        for n, v in enumerate((value,) + shifted_frames(value, behind, ahead)):
            spot = (3 * q + (1, 0, 2)[n]) * chan
            rim[spot : spot + chan, :] = v[:, frame_dev:]
            if q in edge:
                spot = (3 * edge.index(q) + (1, 0, 2)[n]) * chan
                g3[spot : spot + chan, :] = v[:, :frame_dev]
    low[chan : (rows + 1) * chan, :frame_dev] = own_low[...]

    def put(m, lanes, result, pre_one):
        at = slice((m + 1) * chan, (m + 2) * chan)
        _, slope = silu_halves(pre_one * scale[:, lanes] + shift[:, lanes])
        mask = usable[:, lanes] * (0.5 * row_valid(m, rows))
        low[at, lanes] = (result * slope * mask * factor[:, lanes]).astype(BF16)

    pre_one = dot(w1[2 * chan : (rows + 4) * chan, :], x3[:, frame_dev:])
    beside = slice(frame_dev, wide)
    for start in range(0, rows + 2, 2):
        result = dot(wb[...], rim[start * 3 * chan : (start + 4) * 3 * chan, :])
        for n in range(2):
            at = slice((start + n) * chan, (start + n + 1) * chan)
            put(start + n - 1, beside, result[n * chan : (n + 1) * chan], pre_one[at])
    own = slice(0, frame_dev)
    result = dot(wb[...], g3[: 4 * 3 * chan, :])
    put(-1, own, result[:chan], dot(w1[2 * chan : 3 * chan, :], x3[:, :frame_dev]))
    result = dot(wb[...], g3[4 * 3 * chan :, :])
    put(rows, own, result[chan:], dot(w1[(rows + 3) * chan : (rows + 4) * chan, :], x3[:, :frame_dev]))
    row = features[0:1, :]
    lane = iota((1, 128), 1)
    gram = jnp.concatenate(
        [jnp.where(lane < 9, pltpu.roll(row, 128 - 9 * t, 1) if t else row, 0.0) for t in range(9)]
        + [jnp.zeros((7, 128), F32)],
        axis=0,
    )
    single = to_column(row, 16, 81)[0:9]
    k_rows = jnp.concatenate([k1t[...], jnp.zeros((112, chan), F32)], axis=0)
    mean_l, inv_l = stats[chan : chan + 1, :chan], stats[chan + 8 : chan + 9, :chan]
    normed = inv_l * (dot(gram, k_rows, precision=EXACT)[0:9] - single * mean_l)
    normed_taps[0:16] = jnp.concatenate([normed, jnp.zeros((7, chan), F32)], axis=0)
    normed_taps[16:32] = jnp.broadcast_to(to_column(row, 16, 81), (16, chan))
    load.wait()
    first[...] = dot(ws[...], low[...])


def finish(recv, features, stats, k1t, first, ws, w1, x3, normed_taps, params, masks,
           spec_hbm, kernel_one_hbm, kernel_two_hbm, gain_hbm, bias_hbm,
           spec_grad, kernel_one, kernel_two, gain_out, bias_out, sems):
    chan = params.shape[1]
    rows = MEL_ROWS
    wide = x3.shape[1]
    frame_dev = wide - RIM
    usable, behind, ahead = (masks[n : n + 1] for n in range(3))
    total = masks[3:4, 0:1]
    gain = params[0:1]
    count = recv.shape[0] // 14
    share = half_share(count, 9 * chan)
    sums = summed_blocks(recv, count)[0:5]
    ten = jnp.concatenate([sums[:, :chan], sums[:, chan:]], axis=0)
    bias_sum = ten[9:10]
    mean_l, inv_l = stats[chan : chan + 1, :chan], stats[chan + 8 : chan + 9, :chan]
    ten = ten - features[1:2, 0:1] * bias_sum
    k = k1t[0:9]
    gain_sum = inv_l * (jnp.sum(k * ten[0:9], axis=0, keepdims=True) - mean_l * bias_sum)
    gain_out[...] = gain_sum
    bias_out[...] = bias_sum
    factor_l = gain * inv_l
    scale = factor_l * gain_sum / total * inv_l
    scale = jnp.concatenate(
        [scale * row_valid(-1, rows)] + [scale] * rows + [scale * row_valid(rows, rows)], axis=1
    )
    many = 3 * rows

    def in_parts(v, right):
        high = lax.reduce_precision(v, 8, 7)
        v = dot(jnp.concatenate([high, v - high], axis=0).astype(BF16), right)
        return v[:many] + v[many:]

    combined = in_parts(ws[...].astype(F32) * scale, w1[2 * chan : (rows + 4) * chan, :])
    left = [recv[pl.ds(5 + p, count, stride=14), :] for p in range(share)]
    taps = TAPS // 2
    whole = [jnp.concatenate([v[:, h * chan : (h + 1) * chan] for v in left], axis=0)[:taps] for h in range(2)]
    whole = jnp.concatenate(whole, axis=0)
    for t in range(9):
        kernel_two[t] = whole[t * chan : (t + 1) * chan].T
    stores = [pltpu.make_async_copy(kernel_two, kernel_two_hbm, sems.at[4])]
    stores[0].start()
    taken = in_parts(combined, x3[...])
    taps = first[...] - taken
    moved = [taps[rows * b : rows * (b + 1)] for b in range(3)]
    mean_full = mean_l + features[1:2, 0:1] * jnp.sum(k, axis=0, keepdims=True)
    constant = jnp.sum(k * (factor_l * (bias_sum - gain_sum * inv_l * mean_full) / total), axis=1, keepdims=True)
    for a in range(3):
        row = iota((rows, 1), 0) + (a - 1) + lax.axis_index("mel") * rows
        valid = ((row >= 0) & (row < lax.axis_size("mel") * rows)).astype(F32) * usable
        for b in range(3):
            t = 3 * (2 - a) + 2 - b
            moved[b] = moved[b] - constant[t : t + 1] * valid
    result = pltpu.roll(moved[0], 1, 1) * behind + moved[1] + pltpu.roll(moved[2], wide - 1, 1) * ahead
    spec_grad[0] = (result * usable)[:, :frame_dev]
    grad_taps = factor_l * (ten[0:9] - (bias_sum * normed_taps[16:25] + gain_sum * normed_taps[0:9]) / total)
    for i in range(3):
        kernel_one[i] = grad_taps[3 * i : 3 * i + 3]
    outs = ((spec_grad, spec_hbm), (kernel_one, kernel_one_hbm), (gain_out, gain_hbm), (bias_out, bias_hbm))
    wait_all(stores + start_all(*outs, sems=sems))


def run(kernel, outs, scratch, *args, hbm=0, apart=(), flops=10**8, size=4 * 10**6):
    vmem = pl.BlockSpec(memory_space=pltpu.VMEM)
    devices = lax.axis_size("mel") * lax.axis_size("tm")
    specs = []
    args = list(args)
    for n, a in enumerate(args):
        if hbm and n >= len(args) - hbm:
            specs.append(pl.BlockSpec(memory_space=pltpu.HBM))
            args[n] = pltpu.with_memory_space_constraint(a, pltpu.HBM)
        else:
            specs.append(vmem)
            args[n] = pltpu.with_memory_space_constraint(a, pltpu.VMEM)
    return pl.pallas_call(
        kernel,
        out_shape=outs,
        in_specs=specs,
        out_specs=[pl.BlockSpec(memory_space=pltpu.HBM) if n in apart else vmem for n in range(len(outs))],
        scratch_shapes=scratch,
        compiler_params=pltpu.CompilerParams(vmem_limit_bytes=(29 + devices // 32) * 2**20),
        cost_estimate=pl.CostEstimate(flops=flops, bytes_accessed=size, transcendentals=0),
    )(*args)


def shape(dims, dtype=F32):
    return jax.ShapeDtypeStruct(dims, dtype)


def kept(dims, dtype=F32):
    return pltpu.VMEM(dims, dtype)


def far(dims, dtype=F32):
    return pltpu.HBM(dims, dtype)


def exchange(blocks, axes=AXES):
    return lax.all_to_all(blocks, axes, 0, 0, tiled=True)


def exchange_rows(rows, axes=AXES):
    return exchange(rows[:, None, :], axes)[:, 0, :]


def shards(spectrum, clip_bounds, kernel_one, gain_one, bias_one, kernel_two, gain_two, bias_two, pooled_grad):
    _, rows, frame_dev = spectrum.shape
    chan = kernel_two.shape[0]
    n_mel, n_tm = lax.axis_size("mel"), lax.axis_size("tm")
    devices = n_mel * n_tm
    half = frame_dev // 2
    wide = frame_dev + RIM
    mels = n_mel * rows

    packed, own, spec, masks = run(
        pack,
        [
            kept((devices, FIRST, 128), BF16),
            kept(pooled_grad.shape, BF16),
            kept(spectrum.shape, BF16),
            kept((8, wide)),
        ],
        [
            pltpu.SMEM(clip_bounds.shape, jnp.int32),
            pltpu.VMEM((2 * chan, half), F32),
            pltpu.VMEM((devices * FIRST, 128), F32),
            pltpu.SemaphoreType.DMA((3,)),
        ],
        spectrum,
        pooled_grad,
        clip_bounds,
        hbm=3,
    )
    recv = exchange(packed)
    ext = rows + 6
    span = 4 * 3 * chan
    wf, wb, w1, ws, pairs, singles, k1t, params, all_masks, edge_masks, twice, own_rows = run(
        weights,
        [
            kept((2 * chan, span), BF16),
            kept((2 * chan, span), BF16),
            kept((ext * chan, 128), BF16),
            far((rows * 3, (rows + 2) * chan), BF16),
            kept((chan, 128)),
            kept((chan, 128)),
            kept((16, chan)),
            kept((8, chan)),
            kept((3 * n_tm, frame_dev)),
            kept((n_tm * 8, 128)),
            kept((128, 128)),
            kept((chan * rows // 2, half), BF16),
        ],
        [
            pltpu.VMEM((9, chan, chan), BF16),
            pltpu.VMEM((3, 3, chan), BF16),
            pltpu.VMEM((4, 1, chan), F32),
            pltpu.SMEM(clip_bounds.shape, jnp.int32),
            pltpu.VMEM((rows * 3, (rows + 2) * chan), BF16),
            pltpu.VMEM((chan * rows // 2, half), F32),
            pltpu.SemaphoreType.DMA((8,)),
        ],
        own,
        clip_bounds,
        jnp.transpose(kernel_two, (2, 3, 0, 1)).reshape(9, chan, chan),
        jnp.transpose(kernel_one, (1, 2, 0)),
        gain_one[None],
        bias_one[None],
        gain_two[None],
        bias_two[None],
        hbm=7,
        apart=(3,),
    )
    pre_two, payload, act, x3, far_rim, stats_one, features = run(
        forward_one,
        [
            kept((rows * chan, wide)),
            kept((devices, SECOND, 128), BF16),
            kept((ext * 3 * chan, wide), BF16),
            kept((128, wide), BF16),
            kept((BAND, RIM)),
            kept((2 * chan + 16, 128)),
            kept((8, 128)),
        ],
        [
            pltpu.VMEM((ext * chan, wide), F32),
            pltpu.VMEM((devices * FIRST, 128), F32),
            pltpu.VMEM((n_tm * 8, 128), F32),
            pltpu.VMEM((mels + 8, RIM), F32),
            pltpu.VMEM((devices * SECOND, 128), F32),
        ],
        recv,
        spec,
        pairs,
        singles,
        twice,
        w1,
        wf,
        params,
        masks,
        all_masks,
        edge_masks,
    )
    recv = exchange(payload)
    grad, kept_half, sent_half, totals, stats_two = run(
        backward_scaled,
        [
            kept((rows * chan, frame_dev)),
            kept((TAPS // 2 + devices, 128)),
            kept((TAPS // 2 + devices, 128)),
            kept((8, 128)),
            kept((chan + 8, 128)),
        ],
        [
            pltpu.VMEM((rows // 2 * chan, frame_dev), F32),
            pltpu.VMEM((3 * chan + 16, rows * frame_dev), BF16),
            pltpu.VMEM((2, TAPS // 2 + devices, 128), F32),
        ],
        recv,
        pre_two,
        act,
        own_rows,
        params,
        masks,
    )
    received = lax.ppermute(sent_half, "tm", [(i, i ^ 1) for i in range(n_tm)])
    pre_ring, ring, rim, row_pairs = run(
        around,
        [kept((4 * chan, wide)), kept((4 * chan, wide)), kept((rows * chan, RIM)), kept((rows // 2 * chan, frame_dev))],
        [
            pltpu.VMEM(((rows // 2 + 2) * chan, RIM), F32),
            pltpu.VMEM((2 * chan, frame_dev), F32),
            pltpu.VMEM((devices * SECOND, 128), F32),
            pltpu.VMEM((2 * chan, half), F32),
            pltpu.VMEM((4 * 3 * chan, wide), BF16),
        ],
        recv,
        pre_two,
        act,
        w1,
        wf,
        x3,
        far_rim,
        stats_one,
        masks,
        stats_two,
    )
    (payload,) = run(
        pack_sums,
        [kept((devices * (half_share(devices, 9 * chan) + 2), 128))],
        [],
        kept_half,
        received,
        totals,
        rim,
    )
    recv = exchange_rows(payload)
    grad, own_low, payload, totals = run(
        backward,
        [
            kept(((rows + 4) * chan, wide), BF16),
            kept((rows * chan, frame_dev), BF16),
            kept((devices * 14, 128)),
            kept((8, 128)),
        ],
        [
            pltpu.VMEM(((rows + 2) * 3 * chan, frame_dev), BF16),
            pltpu.VMEM((rows * chan, frame_dev), F32),
            pltpu.VMEM((rows * chan, frame_dev), F32),
        ],
        recv,
        pre_two,
        pre_ring,
        grad,
        ring,
        rim,
        stats_two,
        w1,
        x3,
        stats_one,
        params,
        masks,
        wb,
    )
    recv = exchange_rows(payload)
    pooled, gain_two_grad, bias_two_grad = run(
        pool,
        [shape((1, chan, rows // 2, half), BF16), shape((1, chan)), shape((1, chan))],
        [
            pltpu.VMEM((rows // 2 * chan, 128), F32),
        ],
        totals,
        row_pairs,
    )
    first, ws, normed_taps = run(
        transposed,
        [
            kept((rows * 3, wide)),
            kept((rows * 3, (rows + 2) * chan), BF16),
            kept((32, chan)),
        ],
        [
            pltpu.VMEM(((rows + 2) * chan, wide), BF16),
            pltpu.VMEM((8 * 3 * chan, frame_dev), BF16),
            pltpu.VMEM(((rows + 4) * 3 * chan, RIM), BF16),
            pltpu.SemaphoreType.DMA,
        ],
        grad,
        own_low,
        w1,
        wb,
        x3,
        stats_one,
        features,
        k1t,
        params,
        masks,
        ws,
        hbm=1,
    )
    spec_grad, kernel_one_grad, kernel_two_grad, gain_one_grad, bias_one_grad = run(
        finish,
        [
            shape((1, rows, frame_dev)),
            shape((3, 3, chan)),
            shape((9, chan, chan)),
            shape((1, chan)),
            shape((1, chan)),
        ],
        [
            pltpu.VMEM((1, rows, frame_dev), F32),
            pltpu.VMEM((3, 3, chan), F32),
            pltpu.VMEM((9, chan, chan), F32),
            pltpu.VMEM((1, chan), F32),
            pltpu.VMEM((1, chan), F32),
            pltpu.SemaphoreType.DMA((5,)),
        ],
        recv,
        features,
        stats_one,
        k1t,
        first,
        ws,
        w1,
        x3,
        normed_taps,
        params,
        masks,
        apart=range(5),
    )
    kernel_two_grad = jnp.transpose(kernel_two_grad.reshape(3, 3, chan, chan), (2, 3, 0, 1))
    return (
        pooled,
        spec_grad,
        jnp.transpose(kernel_one_grad, (2, 0, 1)),
        gain_one_grad[0],
        bias_one_grad[0],
        kernel_two_grad,
        gain_two_grad[0],
        bias_two_grad[0],
    )


def solution(mesh):
    return jax.shard_map(
        shards,
        mesh=mesh,
        in_specs=(
            P(None, "mel", "tm"),
            P(),
            P(),
            P(),
            P(),
            P(),
            P(),
            P(),
            P(None, None, "mel", "tm"),
        ),
        out_specs=(P(None, None, "mel", "tm"), P(None, "mel", "tm"), P(), P(), P(), P(), P(), P()),
        check_vma=False,
    )
```

```python
import math

import jax
import jax.numpy as jnp
from jax import lax
from jax.experimental import pallas as pl
from jax.experimental.pallas import tpu as pltpu
from jax.sharding import PartitionSpec as P

F32 = jnp.float32
BF16 = jnp.bfloat16
AXES = ("mel", "tm")
EXACT = lax.Precision.HIGHEST
RIM = 128
BAND = 24
MEL_ROWS = 16
FIRST = 16
SUMS, EDGES, COLUMNS = 8, 11, 15
SIDE, FAR = 96, 112
FAR_HOLDERS = 32
LAST = 24
TAPS = 576
SECOND = 8


def iota(shape, dim):
    return lax.broadcasted_iota(jnp.int32, shape, dim)


def dot(a, b, over=((1,), (0,)), precision=None):
    return lax.dot_general(a, b, (over, ((), ())), precision=precision, preferred_element_type=F32)


def to_column(lanes, count, start=0):
    shape = (count, lanes.shape[1])
    return jnp.sum(jnp.where(iota(shape, 1) == iota(shape, 0) + start, lanes, 0.0), axis=1, keepdims=True)


def to_lanes(column, start=0, width=128):
    shape = (column.shape[0], width)
    return jnp.sum(jnp.where(iota(shape, 1) == iota(shape, 0) + start, column, 0.0), axis=0, keepdims=True)


def halves(v):
    total = v[:, :128]
    for n in range(128, v.shape[1], 128):
        total = total + v[:, n : n + 128]
    return total


def frame_masks(bounds, frames):
    last = bounds.shape[1] - 1

    def living(f):
        return (f >= 0) & (f < bounds[0, last])

    def paired(f):
        both = living(f) & living(f + 1)
        for k in range(1, last):
            both = both & (f + 1 != bounds[0, k])
        return both

    return tuple(m.astype(F32) for m in (living(frames), paired(frames - 1), paired(frames)))


def row_valid(row, rows):
    mel = lax.axis_index("mel") * rows + row
    return ((mel >= 0) & (mel < lax.axis_size("mel") * rows)).astype(F32)


def start_all(*pairs, sems):
    copies = [pltpu.make_async_copy(src, dst, sems.at[n]) for n, (src, dst) in enumerate(pairs)]
    for copy in copies:
        copy.start()
    return copies


def wait_all(copies):
    for copy in copies:
        copy.wait()


def shifted_frames(value, behind, ahead):
    wide = value.shape[1]
    return pltpu.roll(value, 1, 1) * behind, pltpu.roll(value, wide - 1, 1) * ahead


def three_parts(v):
    high = lax.reduce_precision(v, 8, 7)
    mid = lax.reduce_precision(v - high, 8, 7)
    return high, mid, v - high - mid


def share_of(devices, chan):
    return -(-chan // devices)


def pack(spec_hbm, grad_hbm, bounds_hbm, out, own, spec, masks, bounds, edges, rows_out, sems):
    copies = start_all((bounds_hbm, bounds), (spec_hbm, spec), (grad_hbm, own), sems=sems)
    copies[0].wait()
    wide = masks.shape[1]
    frame_dev = wide - RIM
    devices = out.shape[0]
    rows = MEL_ROWS
    lane = iota((1, wide), 1)
    frames = lax.axis_index("tm") * frame_dev + jnp.where(lane < frame_dev + RIM // 2, lane, lane - wide)
    last = bounds.shape[1] - 1
    pixels = (bounds[0, last] * (lax.axis_size("mel") * rows)).astype(F32)
    found = frame_masks(bounds, frames)
    masks[...] = jnp.concatenate(
        list(found) + [jnp.full((1, wide), 1.0) * pixels, jnp.zeros((4, wide), F32)], axis=0
    )
    usable, behind, ahead = (m[:, :frame_dev] for m in found)
    copies[1].wait()
    x = spec[0].astype(F32) * usable
    lane = iota((1, frame_dev), 1)
    row = iota((rows, 1), 0)
    inner = jnp.where((lane > 0) & (lane < frame_dev - 1), usable, 0.0)
    number = (rows - 2) * jnp.sum(inner, axis=1, keepdims=True)
    inner = inner * ((row > 0) & (row < rows - 1)).astype(F32)
    centre = jnp.sum(jnp.sum(x, axis=0, keepdims=True), axis=1, keepdims=True)
    centre = centre / (rows * jnp.maximum(jnp.sum(usable, axis=1, keepdims=True), 1.0))
    centre = lax.reduce_precision(centre, 8, 7)
    shifted = [pltpu.roll(x, 1, 1) * behind, x, pltpu.roll(x, frame_dev - 1, 1) * ahead]
    taps = [pltpu.roll(v, (1 - i) % rows, 0) if i != 1 else v for i in range(3) for v in shifted]
    features = feature_rows(centre, (taps, inner))
    lane = iota((1, 128), 1)
    features = jnp.where(lane == 90, centre, jnp.where(lane == 91, number, features))
    pick = iota((8, frame_dev), 0)
    column = jnp.where(pick < 4, pick, frame_dev - 8 + pick)
    strip = dot((iota((8, frame_dev), 1) == column).astype(BF16), x.astype(BF16), ((1,), (1,)))
    lane = iota((8, 128), 1)
    repeat = (iota((rows, 128), 1) % rows == iota((rows, 128), 0)).astype(BF16)
    strip = jnp.where(lane // rows == iota((8, 128), 0), dot(strip.astype(BF16), repeat), 0.0)
    strip = jnp.sum(strip, axis=0, keepdims=True)

    def put(n, value):
        rows_out[pl.ds(n, devices, stride=FIRST), :] = jnp.broadcast_to(value, (devices, 128))

    near = jnp.concatenate([x[0:2], x[rows - 2 :]], axis=0)
    near = jnp.concatenate([near[:, :128], near[:, 128:]], axis=0)
    for d in range(devices):
        rows_out[FIRST * d : FIRST * d + 8, :] = near
    put(COLUMNS, strip)
    copies[2].wait()
    _, chan, many, half = own.shape
    share = share_of(devices, chan)
    holders = chan // share
    g = own[0].astype(F32)
    edges[0:chan] = g[:, 0, :]
    edges[chan:] = g[:, many - 1, :]

    def spread_out(v, held):
        if held < devices:
            v = jnp.concatenate([v, jnp.zeros((devices - held, 128), F32)], axis=0)
        return v

    for n in range(share):
        put(EDGES + n, spread_out(edges[n * holders : (n + 1) * holders, :], holders))
        put(EDGES + share + n, spread_out(edges[chan + n * holders : chan + (n + 1) * holders, :], holders))
    for n in range(2 * share, COLUMNS - EDGES):
        put(EDGES + n, jnp.zeros((1, 128), F32))
    end = iota((8, half), 0)
    at = iota((8, half), 1)
    ends = ((end == 0) & (at == 0)) | ((end == 1) & (at == half - 1))
    columns = dot(ends.astype(BF16), g.reshape(chan * many, half).astype(BF16), ((1,), (1,)))
    group = 128 // many
    source = iota((128, 128), 0)
    lane = iota((group, 128), 1)
    mine = lane // many == iota((group, 128), 0)
    lane8, own8 = iota((8, 128), 1), iota((8, 128), 0)
    parts = three_parts(features)
    for n in range(2):
        side = jnp.zeros((holders, 128), F32)
        for m in range(share):
            move = (iota((128, 128), 1) == SIDE + many * m + source % many).astype(BF16)
            first = m * holders * many // 128
            block = [columns[n : n + 1, 128 * q : 128 * (q + 1)] for q in range(first, first + holders * many // 128)]
            block = jnp.concatenate([jnp.where(mine, v, 0.0) for v in block], axis=0)
            side = side + dot(block.astype(BF16), move)
        far = x[2:4] if n == 0 else x[rows - 4 : rows - 2]
        pieces = [far[r : r + 1, 128 * h : 128 * (h + 1)] for r in range(2) for h in range(2)]
        pieces = jnp.concatenate([jnp.where(lane8 // 16 == own8, v, 0.0) for v in pieces], axis=0)
        far = dot(pieces.astype(BF16), (iota((128, 128), 1) == FAR + source % 16).astype(BF16))
        put(SUMS + n, spread_out(side, holders) + spread_out(far, FAR_HOLDERS) + parts[n])
    put(SUMS + 2, parts[2])
    out[...] = rows_out[...].reshape(out.shape).astype(BF16)


def weights(own, bounds_hbm, k2_hbm, k1_hbm, gain_one_hbm, bias_one_hbm, gain_two_hbm, bias_two_hbm,
            wf, wb, w1, ws_hbm, pairs, singles, k1t, params, all_masks, edge_masks, twice, own_rows,
            k2, k1, vectors, bounds, ws, temp, sems):
    loads = start_all(
        (bounds_hbm, bounds),
        (k2_hbm, k2),
        (k1_hbm, k1),
        (gain_one_hbm, vectors.at[0]),
        (bias_one_hbm, vectors.at[1]),
        (gain_two_hbm, vectors.at[2]),
        (bias_two_hbm, vectors.at[3]),
        sems=sems,
    )
    _, many, count, half = own.shape
    temp[...] = own[0].astype(F32).reshape(many * count, half)
    for r in range(count):
        own_rows[r * many : (r + 1) * many] = temp[pl.ds(r, many, stride=count), :].astype(BF16)
    wait_all(loads)
    chan = k2.shape[1]
    span = wf.shape[1]
    taps = [k2[t].astype(F32) for t in range(9)]
    rest = jnp.zeros((chan, span - 9 * chan), F32)
    forward = jnp.concatenate(taps + [rest], axis=1)
    backward = jnp.concatenate([taps[8 - t].T for t in range(9)] + [rest], axis=1)
    for r in range(wb.shape[0] // chan):
        at = slice(r * chan, (r + 1) * chan)
        wb[at] = (pltpu.roll(backward, 3 * chan * r, 1) if r else backward).astype(BF16)
    full = jnp.concatenate([k1[n].astype(F32) for n in range(3)] + [jnp.zeros((7, chan), F32)], axis=0)
    low = [
        jnp.concatenate([full[3 * (2 - a) + 2 - b : 3 * (2 - a) + 3 - b] for a in range(3)], axis=1)
        for b in range(3)
    ]
    rest = jnp.zeros((1, ws.shape[1] - 3 * chan), F32)
    for b in range(3):
        base = jnp.concatenate([low[b], rest], axis=1)
        many = ws.shape[0] // 3
        rolled = [pltpu.roll(base, chan * m, 1) if m else base for m in range(many)]
        ws[many * b : many * (b + 1)] = jnp.concatenate(rolled, axis=0).astype(BF16)
    store_ws = pltpu.make_async_copy(ws, ws_hbm, sems.at[7])
    store_ws.start()
    count, frame_dev = all_masks.shape[0] // 3, all_masks.shape[1]
    frames = iota((count, frame_dev), 0) * frame_dev + iota((count, frame_dev), 1)
    for n, mask in enumerate(frame_masks(bounds, frames)):
        all_masks[n * count : (n + 1) * count] = mask
    q = iota(edge_masks.shape, 0)
    lane = iota(edge_masks.shape, 1)
    k = q % 8
    frames = (q // 8) * frame_dev + jnp.where(k < 4, k, k + frame_dev - 8)
    living, behind, ahead = frame_masks(bounds, frames)
    living = jnp.where((k == 0) | (k == 7), living, 0.0)
    edge_masks[...] = jnp.where(lane == 0, living, jnp.where(lane == 1, behind, jnp.where(lane == 2, ahead, 0.0)))
    params[...] = jnp.concatenate(
        [vectors[n] for n in range(4)] + [jnp.zeros((4, chan), F32)], axis=0
    )
    tap = iota((16, 128), 0)
    lane = iota((16, 128), 1)
    i = (tap * 11) >> 5
    ninth = (lane * 57) >> 9
    to_band = (lane == BAND * (tap - 3 * i) + i) & (tap < 9)
    to_left = (ninth == tap) & (tap < 9)
    to_right = (lane - 9 * ninth == tap) & (lane < 81)
    to_single = (lane == 81 + tap) & (tap < 9)
    source = iota((128, 128), 0) - 81
    lane = iota((128, 128), 1)
    ninth = (lane * 57) >> 9
    inside = (source >= 0) & (source < 9) & (lane < 81)
    twice[...] = jnp.where(inside, (source == ninth).astype(F32) + (source == lane - 9 * ninth).astype(F32), 0.0)
    for r in range(wf.shape[0] // chan):
        at = slice(r * chan, (r + 1) * chan)
        wf[at] = (pltpu.roll(forward, 3 * chan * r, 1) if r else forward).astype(BF16)
    k1t[...] = full
    k = full.astype(BF16)
    lanes = [dot(k, select.astype(BF16), ((0,), (0,))) for select in (to_band, to_left, to_right, to_single)]
    pairs[...] = lanes[1] * lanes[2]
    singles[...] = lanes[3]
    for m in range(w1.shape[0] // chan):
        w1[m * chan : (m + 1) * chan] = (pltpu.roll(lanes[0], m, 1) if m else lanes[0]).astype(BF16)
    store_ws.wait()


def feature_rows(centre, *parts):
    def folded(v):
        return jnp.sum(halves(v), axis=0, keepdims=True)

    rows = [jnp.zeros((1, 128), F32)] * 96
    for taps, weight in parts:
        z = [tap - centre for tap in taps]
        for s in range(9):
            left = z[s] * weight
            rows[81 + s] = rows[81 + s] + folded(left)
            for t in range(s, 9):
                rows[9 * s + t] = rows[9 * t + s] = rows[9 * s + t] + folded(left * z[t])
    return to_lanes(jnp.sum(jnp.concatenate(rows, axis=0), axis=1, keepdims=True))


def summed_blocks(ref, devices, by=1):
    block = ref.shape[0] // devices
    period = max(8 // math.gcd(block, 8), by)
    step = period * block
    total = ref[0:step, :]
    for at in range(step, ref.shape[0], step):
        total = total + ref[at : at + step, :]
    results = []
    for first in range(by):
        result = total[first * block : (first + 1) * block]
        for n in range(first + by, period, by):
            result = result + total[n * block : (n + 1) * block]
        results.append(result)
    return results if by > 1 else results[0]


def moved_rows(v, step):
    if step == 0:
        return v
    count = v.shape[0]
    if abs(step) >= count:
        return jnp.zeros_like(v)
    zero = jnp.zeros((abs(step), v.shape[1]), v.dtype)
    if step > 0:
        return jnp.concatenate([zero, v[: count - step]], axis=0)
    return jnp.concatenate([v[-step:], zero], axis=0)


def silu_halves(h):
    t = jnp.tanh(h)
    one = 1.0 + t
    return h * one, one * (1.0 + h * (1.0 - t))


def act_row(act, r, low, low_masks):
    low = low * low_masks[0]
    chan = low.shape[0]
    for n, v in enumerate((low,) + shifted_frames(low, *low_masks[1:])):
        at = (3 * r + (1, 0, 2)[n]) * chan
        act[at : at + chan, :] = v


def forward_one(recv, spec, pairs, singles, twice, w1, wf, params, masks, all_masks, edge_masks,
                pre_two, payload, act, x3, far_rim, stats, features_out, pre_one, got, strips, halo, rows_out):
    devices = recv.shape[0]
    n_mel, count = lax.axis_size("mel"), lax.axis_size("tm")
    rows = MEL_ROWS
    mels = n_mel * rows
    wide = masks.shape[1]
    frame_dev = wide - RIM
    chan = params.shape[1]
    me_m, me_t = lax.axis_index("mel"), lax.axis_index("tm")
    usable, behind, ahead = (masks[n : n + 1] for n in range(3))
    total = masks[3:4, 0:1]
    got[...] = recv[...].astype(F32).reshape(devices * FIRST, 128)

    def every(n):
        return got[pl.ds(n, devices, stride=FIRST), :]

    lane = iota((count, 128), 1)
    bands = [got[pl.ds(FIRST * k * count + COLUMNS, count, stride=FIRST), :] for k in range(n_mel)]
    for c in range(8):
        column = jnp.zeros((count, 128), F32)
        for k, band in enumerate(bands):
            part = jnp.where(lane // rows == c, band, 0.0)
            column = column + (pltpu.roll(part, rows * (k - c) % 128, 1) if k != c else part)
        strips[pl.ds(c, count, stride=8), :] = column
    at = pl.multiple_of(FIRST * (jnp.maximum(me_m - 1, 0) * count + me_t), 8)
    above = got[pl.ds(at, 8), :] * (me_m > 0).astype(F32)
    at = pl.multiple_of(FIRST * (jnp.minimum(me_m + 1, n_mel - 1) * count + me_t), 8)
    below = got[pl.ds(at, 8), :] * (me_m < n_mel - 1).astype(F32)
    above = jnp.concatenate([above[2:4], above[6:8]], axis=1)
    below = jnp.concatenate([below[0:2], below[4:6]], axis=1)
    own = spec[0].astype(F32) * usable[:, :frame_dev]
    at = pl.multiple_of(8 * jnp.minimum(me_t + 1, count - 1), 8)
    after = strips[pl.ds(at, 8), :][:, :mels] * (me_t + 1 < count).astype(F32)
    at = pl.multiple_of(8 * jnp.maximum(me_t - 1, 0), 8)
    before = strips[pl.ds(at, 8), :][:, :mels] * (me_t > 0).astype(F32)
    sides = jnp.concatenate([after[0:4], before[4:8], jnp.zeros((8, mels), F32)], axis=0).astype(BF16)
    side = iota((16, RIM), 0)
    place = iota((16, RIM), 1) == jnp.where(side < 4, side, jnp.where(side < 8, side + RIM - 8, -1))
    halo[0:8] = jnp.zeros((8, RIM), F32)
    halo[mels : mels + 8] = jnp.zeros((8, RIM), F32)
    halo[4 : mels + 4] = dot(sides, place.astype(BF16), ((0,), (0,)))
    rim = halo[pl.ds(pl.multiple_of(me_m * rows, 8), BAND), :]
    far_rim[...] = rim
    row = iota((BAND, RIM), 0)
    rim = jnp.where((row >= 2) & (row < BAND - 2), rim, 0.0)
    blank = jnp.zeros((2, frame_dev), F32)
    near = jnp.concatenate([jnp.concatenate([blank, above, own, below, blank], axis=0), rim], axis=1)
    x3[...] = jnp.concatenate(
        [
            pltpu.roll(near, 1, 1) * behind,
            near,
            pltpu.roll(near, wide - 1, 1) * ahead,
            jnp.broadcast_to(usable, (BAND, wide)),
            jnp.zeros((128 - 4 * BAND, wide), F32),
        ],
        axis=0,
    ).astype(BF16)
    pre_one[2 * chan : (rows + 4) * chan] = dot(w1[2 * chan : (rows + 4) * chan, :], x3[...])
    lane = iota((1, 128), 1)
    parts = jnp.where(lane < 92, every(SUMS) + every(SUMS + 1) + every(SUMS + 2), 0.0)
    centres, numbers = parts[:, 90:91], parts[:, 91:92]
    centre = jnp.sum(centres * numbers, axis=0, keepdims=True)
    centre = centre / jnp.maximum(jnp.sum(numbers, axis=0, keepdims=True), 1.0)
    delta = centres - centre
    features = jnp.sum(parts + delta * numbers * jnp.where(lane < 81, delta, 1.0), axis=0, keepdims=True)
    moved = jnp.sum(delta * parts, axis=0, keepdims=True)
    def edge_row(k, n):
        first = FIRST * k * count + n
        return jnp.concatenate(
            [got[pl.ds(first, count, stride=FIRST), :], got[pl.ds(first + 4, count, stride=FIRST), :]], axis=1
        )

    edge_rows = [[edge_row(k, n) for n in range(4)] for k in range(n_mel)]
    zero = jnp.zeros((count, frame_dev), F32)
    rows_of = [[], [], []]
    for k, (top, second, fore, bottom) in enumerate(edge_rows):
        for n, v in enumerate((edge_rows[k - 1][3] if k else zero, top, second)):
            rows_of[n].append(v)
        for n, v in enumerate((fore, bottom, edge_rows[k + 1][0] if k + 1 < n_mel else zero)):
            rows_of[n].append(v)
    f_usable, f_behind, f_ahead = (all_masks[n * count : (n + 1) * count, :] for n in range(3))
    lane = iota((count, frame_dev), 1)

    def frame_before(v):
        v = pltpu.roll(v, 1, 1)
        return jnp.where(lane == 0, pltpu.roll(v, 1, 0), v) * f_behind

    def frame_after(v):
        v = pltpu.roll(v, frame_dev - 1, 1)
        return jnp.where(lane == frame_dev - 1, pltpu.roll(v, count - 1, 0), v) * f_ahead

    taps = []
    for group in rows_of:
        for move in (frame_before, lambda v: v, frame_after):
            taps.append(jnp.concatenate([move(v) for v in group], axis=1))
    f_usable = jnp.concatenate([f_usable] * (2 * n_mel), axis=1)
    borders = (taps, f_usable)
    edge = strips[...]
    q_usable, q_behind, q_ahead = (edge_masks[:, n : n + 1] for n in range(3))
    lane = iota((count * 8, 128), 1)
    inside = (lane < mels) & (lane % rows != 0) & (lane % rows != rows - 1)
    shifted = [
        pltpu.roll(edge, 1, 0) * q_behind,
        edge,
        pltpu.roll(edge, count * 8 - 1, 0) * q_ahead,
    ]
    taps = [pltpu.roll(v, (1 - i) % 128, 1) if i != 1 else v for i in range(3) for v in shifted]
    features = features + feature_rows(centre, borders, (taps, jnp.where(inside, q_usable, 0.0)))
    features = jnp.where(iota((1, 128), 1) < 90, features, 0.0)
    near_mean = jnp.sum(singles[...] * features, axis=1, keepdims=True) / total
    around = jnp.sum(singles[...], axis=1, keepdims=True)
    square = jnp.sum(pairs[...] * features, axis=1, keepdims=True)
    square = (square + 2.0 * around * jnp.sum(singles[...] * moved, axis=1, keepdims=True)) / total
    inv = lax.rsqrt(square - near_mean * near_mean + 1e-05)
    mean = near_mean + centre * around
    lane = iota((chan, 128), 1)
    stats[0:chan] = jnp.where(lane == 0, mean, jnp.where(lane == 1, inv, 0.0))
    stats[chan : chan + 8] = jnp.broadcast_to(to_lanes(near_mean), (8, 128))
    stats[chan + 8 : chan + 16] = jnp.broadcast_to(to_lanes(inv), (8, 128))
    scale = 0.5 * to_column(params[0:1], chan) * inv
    shift = 0.5 * to_column(params[1:2], chan) - mean * scale
    stats[chan + 16 :] = jnp.where(lane == 0, scale, jnp.where(lane == 1, shift, 0.0))
    scale = jnp.broadcast_to(scale, (chan, wide))
    shift = jnp.broadcast_to(shift, (chan, wide))
    block, taps = wf.shape
    first = jnp.zeros((chan, 128), F32)
    second = jnp.zeros((chan, 128), F32)
    own_mask = usable[:, :frame_dev]
    low_masks = [m.astype(BF16) for m in (usable, behind, ahead)]
    for r in range(2, rows + 4):
        value, _ = silu_halves(pre_one[r * chan : (r + 1) * chan, :] * scale + shift)
        if not 0 <= r - 3 < rows:
            value = value * row_valid(r - 3, rows)
        act_row(act, r, value.astype(BF16), low_masks)
        if r < 5 or r % 2 == 0:
            continue
        g = (r - 3) // 2
        result = dot(wf[...], act[g * 3 * block : g * 3 * block + taps, :frame_dev])
        at = (g - 1) * block
        pre_two[at : at + block, :frame_dev] = result
        if g % 2 == 0:
            beside = [act[n * 3 * block : n * 3 * block + taps, frame_dev:] for n in (g - 1, g)]
            beside = dot(wf[...], jnp.concatenate(beside, axis=1))
            for n in range(2):
                pre_two[at + (n - 1) * block : at + n * block, frame_dev:] = beside[:, n * RIM : (n + 1) * RIM]
        for q in range(2):
            p = result[q * chan : (q + 1) * chan]
            masked = p * own_mask
            first = first + halves(masked)
            second = second + halves(masked * p)
    moved = dot(jnp.broadcast_to(moved, (8, 128)), twice[...], precision=EXACT)[0:1]
    features_out[...] = jnp.concatenate(
        [features + moved, jnp.broadcast_to(centre, (1, 128)), jnp.zeros((6, 128), F32)], axis=0
    )
    share = share_of(devices, chan)

    def put(n, value):
        rows_out[pl.ds(n, devices, stride=SECOND), :] = jnp.broadcast_to(value, (devices, 128))

    for n in range(share):
        put(3 + n, moved_rows(every(EDGES + share + n), count))
        put(3 + share + n, moved_rows(every(EDGES + n), -count))
    for n in [0, 1, 2] + list(range(3 + 2 * share, SECOND - 1)):
        put(n, jnp.zeros((1, 128), F32))
    lane = iota((devices, 128), 1)
    tm = iota((devices, 128), 0) % count
    at_side = (lane >= SIDE) & (lane < FAR)
    lefts = jnp.where(at_side, every(SUMS), 0.0)
    rights = jnp.where(at_side, every(SUMS + 1), 0.0)
    beside = jnp.zeros((devices, 128), F32)
    for n, step in enumerate((0, count, -count)):
        one = jnp.where(tm > 0, moved_rows(rights, step + 1), 0.0)
        two = jnp.where(tm < count - 1, moved_rows(lefts, step - 1), 0.0)
        beside = beside + pltpu.roll(one, (32 * n - SIDE) % 128, 1) + pltpu.roll(two, (32 * n + 16 - SIDE) % 128, 1)
    outer = jnp.where(lane >= FAR, moved_rows(every(SUMS + 1), count), 0.0)
    beside = beside + pltpu.roll(outer, 128 - 16, 1)
    beside = beside + jnp.where(lane >= FAR, moved_rows(every(SUMS), -count), 0.0)
    put(SECOND - 1, beside)
    first = jnp.sum(first, axis=1, keepdims=True)
    second = jnp.sum(second, axis=1, keepdims=True)
    parts = list(three_parts(to_lanes(first) + to_lanes(second, chan)))
    parts = jnp.concatenate(parts + [jnp.zeros((SECOND - 3, 128), F32)], axis=0)
    for d in range(devices):
        payload[d] = (rows_out[SECOND * d : SECOND * (d + 1), :] + parts).astype(BF16)


def spreading(half):
    lane = iota((half, 2 * half), 1)
    return jnp.where(lane >> 1 == iota((half, 2 * half), 0), 0.25, 0.0).astype(BF16)


def half_share(devices, taps):
    return -(-taps // 2 // devices)


def backward_scaled(recv, pre_two, act, own_rows, params, masks,
                    grad, kept_half, sent_half, totals, stats, pairs, up, right, halved):
    devices = recv.shape[0]
    chan = params.shape[1]
    half = own_rows.shape[1]
    frame_dev = 2 * half
    rows = MEL_ROWS
    up[...] = dot(own_rows[...], spreading(half))
    usable = masks[0:1, :frame_dev]
    total = masks[3:4, 0:1]
    sums = [recv[d].astype(F32) for d in range(devices)]
    while len(sums) > 1:
        sums = [a + b for a, b in zip(sums[0::2], sums[1::2])]
    sums = jnp.sum(sums[0][0:3], axis=0, keepdims=True)
    mean = to_column(sums, chan) / total
    inv = lax.rsqrt(to_column(sums, chan, chan) / total - mean * mean + 1e-05)
    scale = 0.5 * to_column(params[2:3], chan) * inv
    shift = 0.5 * to_column(params[3:4], chan) - mean * scale
    lane = iota((chan, 128), 1)
    columns = jnp.zeros((chan, 128), F32)
    for n, column in enumerate((mean, inv, scale, shift)):
        columns = jnp.where(lane == n, column, columns)
    stats[0:chan] = columns
    stats[chan : chan + 8] = jnp.broadcast_to(to_lanes(inv), (8, 128))
    mean, inv, scale, shift = (jnp.broadcast_to(v, (chan, frame_dev)) for v in (mean, inv, scale, shift))
    first = jnp.zeros((chan, 128), F32)
    second = jnp.zeros((chan, 128), F32)
    mask = 0.5 * usable
    right[3 * chan :] = jnp.ones((16, rows * frame_dev), BF16)
    table = jnp.zeros((9 * chan, 3 * chan + 16), F32)
    for m in range(rows):
        at = slice(m * chan, (m + 1) * chan)
        pre = pre_two[at, :frame_dev]
        value, slope = silu_halves(pre * scale + shift)
        value = value * usable
        both = value if m % 2 == 0 else both + value
        if m % 2:
            pairs[m // 2 * chan : (m // 2 + 1) * chan, :] = both
        g = up[m // 2 * chan : (m // 2 + 1) * chan, :] * slope * mask
        grad[at, :] = g
        normed = (pre - mean) * inv
        first = first + halves(g * normed)
        second = second + halves(g)
        lanes = slice(m * frame_dev, (m + 1) * frame_dev)
        right[0:chan, lanes] = g.astype(BF16)
        right[chan : 2 * chan, lanes] = normed.astype(BF16)
        right[2 * chan : 3 * chan, lanes] = (g - right[0:chan, lanes].astype(F32)).astype(BF16)
        if m in (5, 11, rows - 1):
            start = m - m % 6
            left = [act[(n + 2) * 3 * chan : (n + 5) * 3 * chan, :frame_dev] for n in range(start, m + 1)]
            lanes = slice(start * frame_dev, (m + 1) * frame_dev)
            table = table + dot(jnp.concatenate(left, axis=1), right[:, lanes], ((1,), (1,)))
    first = jnp.sum(first, axis=1, keepdims=True)
    second = jnp.sum(second, axis=1, keepdims=True)
    totals[...] = jnp.broadcast_to(to_lanes(first) + to_lanes(second, chan), (8, 128))
    rest = jnp.concatenate([table[:, 2 * chan :], jnp.zeros((9 * chan, chan - 16), F32)], axis=1)
    both = table[:, : 2 * chan] + jnp.where(iota(rest.shape, 1) < chan, rest, 0.0)
    single = rest[:, chan : chan + 1]
    taps = 9 * chan // 2
    lane = iota((devices, 128), 1)
    for h in range(2):
        halved[h, 0:taps] = both[h * taps : (h + 1) * taps]
        constants = jnp.zeros((devices, 128), F32)
        for k in range(half_share(devices, 9 * chan)):
            at = h * taps + k * devices
            ones = single[at : min(at + devices, (h + 1) * taps)]
            if ones.shape[0] < devices:
                ones = jnp.concatenate([ones, jnp.zeros((devices - ones.shape[0], 1), F32)], axis=0)
            constants = jnp.where(lane == k, ones, constants)
        halved[h, taps:] = constants
    core = lax.axis_index("tm") % 2
    kept_half[...] = halved[core]
    sent_half[...] = halved[1 - core]


def around(recv, pre_two, act, w1, wf, x3, far_rim, stats_one, masks, stats, pre_ring, ring, rim,
           sides, up, got, beyond, more):
    devices = recv.shape[0]
    got[...] = recv[:, 0:SECOND, :].astype(F32).reshape(devices * SECOND, 128)
    rows = MEL_ROWS
    many = rows // 2
    wide = pre_two.shape[1]
    frame_dev = wide - RIM
    chan = pre_two.shape[0] // rows
    usable = masks[0:1]
    low_masks = [masks[n : n + 1].astype(BF16) for n in range(3)]
    pieces = got[pl.ds(SECOND - 1, devices, stride=SECOND), :][:FAR_HOLDERS].astype(BF16)
    source = iota((128, 128), 0)
    lane = iota((FAR_HOLDERS, 128), 1)
    mine = lane // 16 == iota((FAR_HOLDERS, 128), 0) % 8
    outer = []
    for first in (SIDE, FAR):
        place = (source - first == iota((128, 128), 1) % 16).astype(BF16)
        v = jnp.where(mine, dot(pieces, place), 0.0)
        v = [jnp.sum(v[8 * n : 8 * n + 8], axis=0, keepdims=True) for n in range(4)]
        outer += [jnp.concatenate(v[2 * r : 2 * r + 2], axis=1) for r in range(2)]
    blank = jnp.zeros((BAND - 4, frame_dev), F32)
    far = jnp.concatenate(outer[:2] + [blank] + outer[2:], axis=0)
    row = iota((BAND, RIM), 0)
    far = jnp.concatenate([far, jnp.where((row < 2) | (row >= BAND - 2), far_rim[...], 0.0)], axis=1)
    far = jnp.concatenate(
        [
            pltpu.roll(far, 1, 1) * masks[1:2],
            far,
            pltpu.roll(far, wide - 1, 1) * masks[2:3],
            jnp.zeros((128 - 3 * BAND, wide), F32),
        ],
        axis=0,
    )
    x_all = (x3[...].astype(F32) + far).astype(BF16)
    scale = jnp.broadcast_to(stats_one[chan + 16 :, 0:1], (chan, wide))
    shift = jnp.broadcast_to(stats_one[chan + 16 :, 1:2], (chan, wide))
    for h, start in enumerate((0, rows + 4)):
        pre_one = dot(w1[start * chan : (start + 2) * chan, :], x_all)
        for n in range(2):
            value, _ = silu_halves(pre_one[n * chan : (n + 1) * chan] * scale + shift)
            value = value * row_valid(start + n - 3, rows)
            act_row(more, 2 * h + n, value.astype(BF16), low_masks)
    line = 3 * chan
    above = jnp.concatenate([more[0 : 2 * line, :], act[2 * line : 4 * line, :]], axis=0)
    below = jnp.concatenate([act[(rows + 2) * line : (rows + 4) * line, :], more[2 * line :, :]], axis=0)
    pre_ring[0 : 2 * chan] = dot(wf[...], above)
    pre_ring[2 * chan :] = dot(wf[...], below)
    share = share_of(devices, chan)
    holders = chan // share

    def every(n):
        return got[pl.ds(n, devices, stride=SECOND), :]

    beside = 0.25 * every(SECOND - 1)[:holders]
    lane = iota((holders, RIM), 1)
    for n in range(share):
        first = n * holders
        beyond[first : first + holders, :] = every(3 + n)[:holders]
        beyond[chan + first : chan + first + holders, :] = every(3 + share + n)[:holders]
        for r in range(many + 2):
            at = many * n + (r if r < many else 32 + many - 1 if r == many else 64)
            left, right_of = beside[:, at : at + 1], beside[:, at + 16 : at + 17]
            side = jnp.where(lane >= RIM - 2, left, jnp.where(lane < 2, right_of, 0.0))
            sides[r * chan + first : r * chan + first + holders, :] = side
    up[...] = dot(beyond[...].astype(BF16), spreading(frame_dev // 2))
    scale = jnp.broadcast_to(stats[0:chan, 2:3], (chan, wide))
    shift = jnp.broadcast_to(stats[0:chan, 3:4], (chan, wide))
    for n, m in enumerate((-2, -1, rows, rows + 1)):
        below = n // 2
        upstream = jnp.concatenate(
            [
                up[below * chan : (below + 1) * chan, :],
                sides[(many + below) * chan : (many + below + 1) * chan, :],
            ],
            axis=1,
        )
        _, slope = silu_halves(pre_ring[n * chan : (n + 1) * chan, :] * scale + shift)
        ring[n * chan : (n + 1) * chan, :] = upstream * slope * (usable * (0.5 * row_valid(m, rows)))
    for m in range(rows):
        at = slice(m * chan, (m + 1) * chan)
        _, slope = silu_halves(pre_two[at, frame_dev:] * scale[:, frame_dev:] + shift[:, frame_dev:])
        upstream = sides[m // 2 * chan : (m // 2 + 1) * chan, :]
        rim[m * chan : (m + 1) * chan, :] = upstream * slope * (0.5 * usable[:, frame_dev:])


def pack_sums(kept_half, received, totals, after, payload):
    del after
    devices = kept_half.shape[0] - TAPS // 2
    block = payload.shape[0] // devices
    payload[pl.ds(0, devices, stride=block), :] = jnp.broadcast_to(totals[0:1], (devices, 128))
    taps = TAPS // 2
    total = kept_half[...] + received[...]
    for k in range(block - 2):
        cut = total[k * devices : min((k + 1) * devices, taps)]
        if cut.shape[0] < devices:
            cut = jnp.concatenate([cut, jnp.zeros((devices - cut.shape[0], 128), F32)], axis=0)
        payload[pl.ds(1 + k, devices, stride=block), :] = cut
    payload[pl.ds(block - 1, devices, stride=block), :] = total[taps:]


def pool(totals, pairs, out, gain_out, bias_out, temp):
    gain_out[...] = totals[0:1, : gain_out.shape[1]]
    bias_out[...] = totals[0:1, gain_out.shape[1] :]
    chan, rows, half = out.shape[1:]
    to_mean = jnp.where(iota((2 * half, half), 0) >> 1 == iota((2 * half, half), 1), 0.25, 0.0)
    pooled = dot(pairs[...], to_mean, precision=EXACT)
    for r in range(rows):
        temp[pl.ds(r, chan, stride=rows), :] = pooled[r * chan : (r + 1) * chan]
    out[0] = temp[...].reshape(chan, rows, half).astype(BF16)


def backward(recv, pre_two, pre_ring, grad, ring, rim, stats_two, w1, x3, stats, params, masks, wb,
             out, own_low, payload, totals, g3, pre_one, g1):
    chan = params.shape[1]
    rows = MEL_ROWS
    wide = pre_two.shape[1]
    frame_dev = wide - RIM
    usable = masks[0:1]
    behind, ahead = (masks[n : n + 1].astype(BF16) for n in (1, 2))
    total = masks[3:4, 0:1]
    devices = payload.shape[0]
    pre_one[...] = dot(w1[3 * chan : (rows + 3) * chan], x3[:, :frame_dev])

    even, odd = summed_blocks(recv, devices, 2)
    sums = even[0:1] + odd[0:1]
    gain_sum, bias_sum = sums[:, :chan], sums[:, chan:]
    totals[...] = jnp.broadcast_to(sums, (8, 128))
    mean, inv = stats_two[0:chan, 0:1], stats_two[0:chan, 1:2]
    factor = to_column(params[2:3], chan) * inv
    gain_part = factor * (to_column(sums, chan) / total * inv)
    bias_part = factor * (to_column(sums, chan, chan) / total) - mean * gain_part
    gain_part = jnp.broadcast_to(gain_part, (chan, wide))
    bias_part = jnp.broadcast_to(bias_part, (chan, wide))
    factor = jnp.broadcast_to(factor, (chan, wide))
    scale = jnp.broadcast_to(stats[chan + 16 :, 0:1], (chan, frame_dev))
    shift = jnp.broadcast_to(stats[chan + 16 :, 1:2], (chan, frame_dev))
    factor_one = jnp.broadcast_to(to_column(params[0:1], chan) * stats[0:chan, 1:2], (chan, frame_dev))
    own_mask = 0.5 * usable[:, :frame_dev]
    count = rows + 4
    share = even.shape[0] - 2
    mine = jnp.concatenate([even[1 : share + 1], odd[1 : share + 1]], axis=0)
    single = jnp.concatenate([to_column(v[share + 1 :], share) for v in (even, odd)], axis=0)
    factor_l = params[2:3] * stats_two[chan : chan + 1, :chan]
    mine = mine[:, :chan] - (bias_sum * single + gain_sum * mine[:, chan:]) / total
    mine = factor_l * mine
    mine = jnp.concatenate([mine[:share], mine[share:]], axis=1)
    if share < 9:
        mine = jnp.concatenate([mine, jnp.zeros((9 - share, 128), F32)], axis=0)
    table = jnp.zeros((chan, 128), F32)

    def tap_sums(m):
        part = g1[m * chan : (m + 4) * chan, :]
        high = lax.reduce_precision(part, 8, 7)
        low = (part - high).astype(BF16)
        taps_in = x3[:, :frame_dev]
        products = dot(high.astype(BF16), taps_in, ((1,), (1,))) + dot(low, taps_in, ((1,), (1,)))
        moved = [pltpu.roll(products[k * chan : (k + 1) * chan], 128 - (m + k + 3), 1) for k in range(4)]
        return (moved[0] + moved[1]) + (moved[2] + moved[3])

    for q in range(count):
        at = slice(q * chan, (q + 1) * chan)
        mask = usable if 0 <= q - 2 < rows else usable * row_valid(q - 2, rows)
        if 2 <= q < rows + 2:
            own = slice((q - 2) * chan, (q - 1) * chan)
            pre, scaled = pre_two[own, :], jnp.concatenate([grad[own, :], rim[own, :]], axis=1)
        else:
            n = q if q < 2 else q - rows
            pre, scaled = pre_ring[n * chan : (n + 1) * chan, :], ring[n * chan : (n + 1) * chan, :]
        low = (factor * scaled - (bias_part + pre * gain_part) * mask).astype(BF16)
        out[at, :] = low
        if not 1 <= q < count - 1:
            continue
        base = (q - 1) * 3 * chan
        for n, v in enumerate((low,) + shifted_frames(low, behind, ahead)):
            spot = base + (1, 0, 2)[n] * chan
            g3[spot : spot + chan, :] = v[:, :frame_dev]
        start = q - 4
        if start < 0 or start % 2:
            continue
        result = dot(wb[...], g3[start * 3 * chan : (start + 4) * 3 * chan, :])
        for n in range(2):
            m = start + n
            at = slice(m * chan, (m + 1) * chan)
            _, slope = silu_halves(pre_one[at, :] * scale + shift)
            value = result[n * chan : (n + 1) * chan] * slope * own_mask
            own_low[at, :] = (value * factor_one).astype(BF16)
            g1[at, :] = value
        if start % 4 == 2 and start > 2:
            table = table + tap_sums(start - 6)
    table = table + tap_sums(rows - 4)
    table = table.T
    places = [BAND * j + i for i in range(3) for j in range(3)] + [3 * BAND]
    rows10 = jnp.concatenate([table[n : n + 1] for n in places], axis=0)
    sums = jnp.concatenate([rows10[0:5], rows10[5:10]], axis=1)
    block = jnp.concatenate(list(three_parts(sums)) + [mine], axis=0).astype(BF16)
    for d in range(devices):
        payload[d] = block


def transposed(grad, own_low, w1, wb, x3, stats, features, k1t, params, masks, ws_hbm,
               first, ws, normed_taps, low, g3, rim, sem):
    load = pltpu.make_async_copy(ws_hbm, ws, sem)
    load.start()
    rows = MEL_ROWS
    chan = own_low.shape[0] // rows
    wide = grad.shape[1]
    frame_dev = wide - RIM
    count = grad.shape[0] // chan
    usable = masks[0:1]
    behind, ahead = (masks[n : n + 1].astype(BF16) for n in (1, 2))
    scale = jnp.broadcast_to(stats[chan + 16 :, 0:1], (chan, wide))
    shift = jnp.broadcast_to(stats[chan + 16 :, 1:2], (chan, wide))
    factor = jnp.broadcast_to(to_column(params[0:1], chan) * stats[0:chan, 1:2], (chan, wide))
    edge = (0, 1, 2, 3, count - 4, count - 3, count - 2, count - 1)
    for q in range(count):
        value = grad[q * chan : (q + 1) * chan, :]
        for n, v in enumerate((value,) + shifted_frames(value, behind, ahead)):
            spot = (3 * q + (1, 0, 2)[n]) * chan
            rim[spot : spot + chan, :] = v[:, frame_dev:]
            if q in edge:
                spot = (3 * edge.index(q) + (1, 0, 2)[n]) * chan
                g3[spot : spot + chan, :] = v[:, :frame_dev]
    low[chan : (rows + 1) * chan, :frame_dev] = own_low[...]

    def put(m, lanes, result, pre_one):
        at = slice((m + 1) * chan, (m + 2) * chan)
        _, slope = silu_halves(pre_one * scale[:, lanes] + shift[:, lanes])
        mask = usable[:, lanes] * (0.5 * row_valid(m, rows))
        low[at, lanes] = (result * slope * mask * factor[:, lanes]).astype(BF16)

    pre_one = dot(w1[2 * chan : (rows + 4) * chan, :], x3[:, frame_dev:])
    beside = slice(frame_dev, wide)
    for start in range(0, rows + 2, 2):
        result = dot(wb[...], rim[start * 3 * chan : (start + 4) * 3 * chan, :])
        for n in range(2):
            at = slice((start + n) * chan, (start + n + 1) * chan)
            put(start + n - 1, beside, result[n * chan : (n + 1) * chan], pre_one[at])
    own = slice(0, frame_dev)
    result = dot(wb[...], g3[: 4 * 3 * chan, :])
    put(-1, own, result[:chan], dot(w1[2 * chan : 3 * chan, :], x3[:, :frame_dev]))
    result = dot(wb[...], g3[4 * 3 * chan :, :])
    put(rows, own, result[chan:], dot(w1[(rows + 3) * chan : (rows + 4) * chan, :], x3[:, :frame_dev]))
    row = features[0:1, :]
    lane = iota((1, 128), 1)
    gram = jnp.concatenate(
        [jnp.where(lane < 9, pltpu.roll(row, 128 - 9 * t, 1) if t else row, 0.0) for t in range(9)]
        + [jnp.zeros((7, 128), F32)],
        axis=0,
    )
    single = to_column(row, 16, 81)[0:9]
    k_rows = jnp.concatenate([k1t[...], jnp.zeros((112, chan), F32)], axis=0)
    mean_l, inv_l = stats[chan : chan + 1, :chan], stats[chan + 8 : chan + 9, :chan]
    normed = inv_l * (dot(gram, k_rows, precision=EXACT)[0:9] - single * mean_l)
    normed_taps[0:16] = jnp.concatenate([normed, jnp.zeros((7, chan), F32)], axis=0)
    normed_taps[16:32] = jnp.broadcast_to(to_column(row, 16, 81), (16, chan))
    load.wait()
    first[...] = dot(ws[...], low[...])


def finish(recv, features, stats, k1t, first, ws, w1, x3, normed_taps, params, masks,
           spec_hbm, kernel_one_hbm, kernel_two_hbm, gain_hbm, bias_hbm,
           spec_grad, kernel_one, kernel_two, gain_out, bias_out, got, sems):
    chan = params.shape[1]
    rows = MEL_ROWS
    wide = x3.shape[1]
    frame_dev = wide - RIM
    usable, behind, ahead = (masks[n : n + 1] for n in range(3))
    total = masks[3:4, 0:1]
    gain = params[0:1]
    count = recv.shape[0]
    share = half_share(count, 9 * chan)
    got[...] = recv[...].astype(F32).reshape(count * LAST, 128)
    sums = summed_blocks(got, count)
    sums = sums[0:5] + sums[5:10] + sums[10:15]
    ten = jnp.concatenate([sums[:, :chan], sums[:, chan:]], axis=0)
    bias_sum = ten[9:10]
    mean_l, inv_l = stats[chan : chan + 1, :chan], stats[chan + 8 : chan + 9, :chan]
    ten = ten - features[1:2, 0:1] * bias_sum
    k = k1t[0:9]
    gain_sum = inv_l * (jnp.sum(k * ten[0:9], axis=0, keepdims=True) - mean_l * bias_sum)
    gain_out[...] = gain_sum
    bias_out[...] = bias_sum
    factor_l = gain * inv_l
    scale = factor_l * gain_sum / total * inv_l
    scale = jnp.concatenate(
        [scale * row_valid(-1, rows)] + [scale] * rows + [scale * row_valid(rows, rows)], axis=1
    )
    many = 3 * rows

    def in_parts(v, right):
        high = lax.reduce_precision(v, 8, 7)
        v = dot(jnp.concatenate([high, v - high], axis=0).astype(BF16), right)
        return v[:many] + v[many:]

    combined = in_parts(ws[...].astype(F32) * scale, w1[2 * chan : (rows + 4) * chan, :])
    left = [got[pl.ds(15 + p, count, stride=LAST), :] for p in range(share)]
    taps = TAPS // 2
    whole = [jnp.concatenate([v[:, h * chan : (h + 1) * chan] for v in left], axis=0)[:taps] for h in range(2)]
    whole = jnp.concatenate(whole, axis=0)
    for t in range(9):
        kernel_two[t] = whole[t * chan : (t + 1) * chan].T
    stores = [pltpu.make_async_copy(kernel_two, kernel_two_hbm, sems.at[4])]
    stores[0].start()
    taken = in_parts(combined, x3[...])
    taps = first[...] - taken
    moved = [taps[rows * b : rows * (b + 1)] for b in range(3)]
    mean_full = mean_l + features[1:2, 0:1] * jnp.sum(k, axis=0, keepdims=True)
    constant = jnp.sum(k * (factor_l * (bias_sum - gain_sum * inv_l * mean_full) / total), axis=1, keepdims=True)
    for a in range(3):
        row = iota((rows, 1), 0) + (a - 1) + lax.axis_index("mel") * rows
        valid = ((row >= 0) & (row < lax.axis_size("mel") * rows)).astype(F32) * usable
        for b in range(3):
            t = 3 * (2 - a) + 2 - b
            moved[b] = moved[b] - constant[t : t + 1] * valid
    result = pltpu.roll(moved[0], 1, 1) * behind + moved[1] + pltpu.roll(moved[2], wide - 1, 1) * ahead
    spec_grad[0] = (result * usable)[:, :frame_dev]
    grad_taps = factor_l * (ten[0:9] - (bias_sum * normed_taps[16:25] + gain_sum * normed_taps[0:9]) / total)
    for i in range(3):
        kernel_one[i] = grad_taps[3 * i : 3 * i + 3]
    outs = ((spec_grad, spec_hbm), (kernel_one, kernel_one_hbm), (gain_out, gain_hbm), (bias_out, bias_hbm))
    wait_all(stores + start_all(*outs, sems=sems))


def run(kernel, outs, scratch, *args, hbm=0, apart=(), flops=10**8, size=4 * 10**6):
    vmem = pl.BlockSpec(memory_space=pltpu.VMEM)
    devices = lax.axis_size("mel") * lax.axis_size("tm")
    specs = []
    args = list(args)
    for n, a in enumerate(args):
        if hbm and n >= len(args) - hbm:
            specs.append(pl.BlockSpec(memory_space=pltpu.HBM))
            args[n] = pltpu.with_memory_space_constraint(a, pltpu.HBM)
        else:
            specs.append(vmem)
            args[n] = pltpu.with_memory_space_constraint(a, pltpu.VMEM)
    return pl.pallas_call(
        kernel,
        out_shape=outs,
        in_specs=specs,
        out_specs=[pl.BlockSpec(memory_space=pltpu.HBM) if n in apart else vmem for n in range(len(outs))],
        scratch_shapes=scratch,
        compiler_params=pltpu.CompilerParams(vmem_limit_bytes=(29 + devices // 32) * 2**20),
        cost_estimate=pl.CostEstimate(flops=flops, bytes_accessed=size, transcendentals=0),
    )(*args)


def shape(dims, dtype=F32):
    return jax.ShapeDtypeStruct(dims, dtype)


def kept(dims, dtype=F32):
    return pltpu.VMEM(dims, dtype)


def far(dims, dtype=F32):
    return pltpu.HBM(dims, dtype)


def exchange(blocks, axes=AXES):
    return lax.all_to_all(blocks, axes, 0, 0, tiled=True)


def exchange_rows(rows, axes=AXES):
    return exchange(rows[:, None, :], axes)[:, 0, :]


def shards(spectrum, clip_bounds, kernel_one, gain_one, bias_one, kernel_two, gain_two, bias_two, pooled_grad):
    _, rows, frame_dev = spectrum.shape
    chan = kernel_two.shape[0]
    n_mel, n_tm = lax.axis_size("mel"), lax.axis_size("tm")
    devices = n_mel * n_tm
    half = frame_dev // 2
    wide = frame_dev + RIM
    mels = n_mel * rows

    packed, own, spec, masks = run(
        pack,
        [
            kept((devices, FIRST, 128), BF16),
            kept(pooled_grad.shape, BF16),
            kept(spectrum.shape, BF16),
            kept((8, wide)),
        ],
        [
            pltpu.SMEM(clip_bounds.shape, jnp.int32),
            pltpu.VMEM((2 * chan, half), F32),
            pltpu.VMEM((devices * FIRST, 128), F32),
            pltpu.SemaphoreType.DMA((3,)),
        ],
        spectrum,
        pooled_grad,
        clip_bounds,
        hbm=3,
    )
    recv = exchange(packed)
    ext = rows + 6
    span = 4 * 3 * chan
    wf, wb, w1, ws, pairs, singles, k1t, params, all_masks, edge_masks, twice, own_rows = run(
        weights,
        [
            kept((2 * chan, span), BF16),
            kept((2 * chan, span), BF16),
            kept((ext * chan, 128), BF16),
            far((rows * 3, (rows + 2) * chan), BF16),
            kept((chan, 128)),
            kept((chan, 128)),
            kept((16, chan)),
            kept((8, chan)),
            kept((3 * n_tm, frame_dev)),
            kept((n_tm * 8, 128)),
            kept((128, 128)),
            kept((chan * rows // 2, half), BF16),
        ],
        [
            pltpu.VMEM((9, chan, chan), BF16),
            pltpu.VMEM((3, 3, chan), BF16),
            pltpu.VMEM((4, 1, chan), F32),
            pltpu.SMEM(clip_bounds.shape, jnp.int32),
            pltpu.VMEM((rows * 3, (rows + 2) * chan), BF16),
            pltpu.VMEM((chan * rows // 2, half), F32),
            pltpu.SemaphoreType.DMA((8,)),
        ],
        own,
        clip_bounds,
        jnp.transpose(kernel_two, (2, 3, 0, 1)).reshape(9, chan, chan),
        jnp.transpose(kernel_one, (1, 2, 0)),
        gain_one[None],
        bias_one[None],
        gain_two[None],
        bias_two[None],
        hbm=7,
        apart=(3,),
    )
    pre_two, payload, act, x3, far_rim, stats_one, features = run(
        forward_one,
        [
            kept((rows * chan, wide)),
            kept((devices, SECOND, 128), BF16),
            kept((ext * 3 * chan, wide), BF16),
            kept((128, wide), BF16),
            kept((BAND, RIM)),
            kept((2 * chan + 16, 128)),
            kept((8, 128)),
        ],
        [
            pltpu.VMEM((ext * chan, wide), F32),
            pltpu.VMEM((devices * FIRST, 128), F32),
            pltpu.VMEM((n_tm * 8, 128), F32),
            pltpu.VMEM((mels + 8, RIM), F32),
            pltpu.VMEM((devices * SECOND, 128), F32),
        ],
        recv,
        spec,
        pairs,
        singles,
        twice,
        w1,
        wf,
        params,
        masks,
        all_masks,
        edge_masks,
    )
    recv = exchange(payload)
    grad, kept_half, sent_half, totals, stats_two, row_pairs = run(
        backward_scaled,
        [
            kept((rows * chan, frame_dev)),
            kept((TAPS // 2 + devices, 128)),
            kept((TAPS // 2 + devices, 128)),
            kept((8, 128)),
            kept((chan + 8, 128)),
            kept((rows // 2 * chan, frame_dev)),
        ],
        [
            pltpu.VMEM((rows // 2 * chan, frame_dev), F32),
            pltpu.VMEM((3 * chan + 16, rows * frame_dev), BF16),
            pltpu.VMEM((2, TAPS // 2 + devices, 128), F32),
        ],
        recv,
        pre_two,
        act,
        own_rows,
        params,
        masks,
    )
    received = lax.ppermute(sent_half, "tm", [(i, i ^ 1) for i in range(n_tm)])
    pre_ring, ring, rim = run(
        around,
        [kept((4 * chan, wide)), kept((4 * chan, wide)), kept((rows * chan, RIM))],
        [
            pltpu.VMEM(((rows // 2 + 2) * chan, RIM), F32),
            pltpu.VMEM((2 * chan, frame_dev), F32),
            pltpu.VMEM((devices * SECOND, 128), F32),
            pltpu.VMEM((2 * chan, half), F32),
            pltpu.VMEM((4 * 3 * chan, wide), BF16),
        ],
        recv,
        pre_two,
        act,
        w1,
        wf,
        x3,
        far_rim,
        stats_one,
        masks,
        stats_two,
    )
    (payload,) = run(
        pack_sums,
        [kept((devices * (half_share(devices, 9 * chan) + 2), 128))],
        [],
        kept_half,
        received,
        totals,
        rim,
    )
    recv = exchange_rows(payload)
    grad, own_low, payload, totals = run(
        backward,
        [
            kept(((rows + 4) * chan, wide), BF16),
            kept((rows * chan, frame_dev), BF16),
            kept((devices, LAST, 128), BF16),
            kept((8, 128)),
        ],
        [
            pltpu.VMEM(((rows + 2) * 3 * chan, frame_dev), BF16),
            pltpu.VMEM((rows * chan, frame_dev), F32),
            pltpu.VMEM((rows * chan, frame_dev), F32),
        ],
        recv,
        pre_two,
        pre_ring,
        grad,
        ring,
        rim,
        stats_two,
        w1,
        x3,
        stats_one,
        params,
        masks,
        wb,
    )
    recv = exchange(payload)
    pooled, gain_two_grad, bias_two_grad = run(
        pool,
        [shape((1, chan, rows // 2, half), BF16), shape((1, chan)), shape((1, chan))],
        [
            pltpu.VMEM((rows // 2 * chan, 128), F32),
        ],
        totals,
        row_pairs,
    )
    first, ws, normed_taps = run(
        transposed,
        [
            kept((rows * 3, wide)),
            kept((rows * 3, (rows + 2) * chan), BF16),
            kept((32, chan)),
        ],
        [
            pltpu.VMEM(((rows + 2) * chan, wide), BF16),
            pltpu.VMEM((8 * 3 * chan, frame_dev), BF16),
            pltpu.VMEM(((rows + 4) * 3 * chan, RIM), BF16),
            pltpu.SemaphoreType.DMA,
        ],
        grad,
        own_low,
        w1,
        wb,
        x3,
        stats_one,
        features,
        k1t,
        params,
        masks,
        ws,
        hbm=1,
    )
    spec_grad, kernel_one_grad, kernel_two_grad, gain_one_grad, bias_one_grad = run(
        finish,
        [
            shape((1, rows, frame_dev)),
            shape((3, 3, chan)),
            shape((9, chan, chan)),
            shape((1, chan)),
            shape((1, chan)),
        ],
        [
            pltpu.VMEM((1, rows, frame_dev), F32),
            pltpu.VMEM((3, 3, chan), F32),
            pltpu.VMEM((9, chan, chan), F32),
            pltpu.VMEM((1, chan), F32),
            pltpu.VMEM((1, chan), F32),
            pltpu.VMEM((devices * LAST, 128), F32),
            pltpu.SemaphoreType.DMA((5,)),
        ],
        recv,
        features,
        stats_one,
        k1t,
        first,
        ws,
        w1,
        x3,
        normed_taps,
        params,
        masks,
        apart=range(5),
    )
    kernel_two_grad = jnp.transpose(kernel_two_grad.reshape(3, 3, chan, chan), (2, 3, 0, 1))
    return (
        pooled,
        spec_grad,
        jnp.transpose(kernel_one_grad, (2, 0, 1)),
        gain_one_grad[0],
        bias_one_grad[0],
        kernel_two_grad,
        gain_two_grad[0],
        bias_two_grad[0],
    )


def solution(mesh):
    return jax.shard_map(
        shards,
        mesh=mesh,
        in_specs=(
            P(None, "mel", "tm"),
            P(),
            P(),
            P(),
            P(),
            P(),
            P(),
            P(),
            P(None, None, "mel", "tm"),
        ),
        out_specs=(P(None, None, "mel", "tm"), P(None, "mel", "tm"), P(), P(), P(), P(), P(), P()),
        check_vma=False,
    )
```

```python
import math

import jax
import jax.numpy as jnp
from jax import lax
from jax.experimental import pallas as pl
from jax.experimental.pallas import tpu as pltpu
from jax.sharding import PartitionSpec as P

F32 = jnp.float32
BF16 = jnp.bfloat16
AXES = ("mel", "tm")
EXACT = lax.Precision.HIGHEST
RIM = 128
BAND = 24
MEL_ROWS = 16
FIRST = 16
SUMS, EDGES, COLUMNS = 8, 11, 15
SIDE, FAR = 96, 112
FAR_HOLDERS = 32
LAST = 24
TAPS = 576
SECOND = 8


def iota(shape, dim):
    return lax.broadcasted_iota(jnp.int32, shape, dim)


def dot(a, b, over=((1,), (0,)), precision=None):
    return lax.dot_general(a, b, (over, ((), ())), precision=precision, preferred_element_type=F32)


def to_column(lanes, count, start=0):
    shape = (count, lanes.shape[1])
    return jnp.sum(jnp.where(iota(shape, 1) == iota(shape, 0) + start, lanes, 0.0), axis=1, keepdims=True)


def to_lanes(column, start=0, width=128):
    shape = (column.shape[0], width)
    return jnp.sum(jnp.where(iota(shape, 1) == iota(shape, 0) + start, column, 0.0), axis=0, keepdims=True)


def halves(v):
    total = v[:, :128]
    for n in range(128, v.shape[1], 128):
        total = total + v[:, n : n + 128]
    return total


def frame_masks(bounds, frames):
    last = bounds.shape[1] - 1
    end = bounds[:, last:]

    def living(f):
        return (f >= 0) & (f < end)

    def paired(f):
        both = living(f) & living(f + 1)
        for k in range(1, last):
            both = both & (f + 1 != bounds[:, k : k + 1])
        return both

    return tuple(m.astype(F32) for m in (living(frames), paired(frames - 1), paired(frames)))


def row_valid(row, rows):
    mel = lax.axis_index("mel") * rows + row
    return ((mel >= 0) & (mel < lax.axis_size("mel") * rows)).astype(F32)


def start_all(*pairs, sems):
    copies = [pltpu.make_async_copy(src, dst, sems.at[n]) for n, (src, dst) in enumerate(pairs)]
    for copy in copies:
        copy.start()
    return copies


def wait_all(copies):
    for copy in copies:
        copy.wait()


def shifted_frames(value, behind, ahead):
    wide = value.shape[1]
    return pltpu.roll(value, 1, 1) * behind, pltpu.roll(value, wide - 1, 1) * ahead


def three_parts(v):
    high = lax.reduce_precision(v, 8, 7)
    mid = lax.reduce_precision(v - high, 8, 7)
    return high, mid, v - high - mid


def share_of(devices, chan):
    return -(-chan // devices)


def pack(spec_hbm, grad_hbm, bounds_hbm, out, own, spec, masks, bounds, edges, rows_out, sems):
    copies = start_all((bounds_hbm, bounds), (spec_hbm, spec), (grad_hbm, own), sems=sems)
    copies[0].wait()
    wide = masks.shape[1]
    frame_dev = wide - RIM
    devices = out.shape[0]
    rows = MEL_ROWS
    lane = iota((1, wide), 1)
    frames = lax.axis_index("tm") * frame_dev + jnp.where(lane < frame_dev + RIM // 2, lane, lane - wide)
    last = bounds.shape[1] - 1
    pixels = bounds[:, last:].astype(F32) * (lax.axis_size("mel") * rows)
    found = frame_masks(bounds[...], frames)
    masks[...] = jnp.concatenate(
        list(found) + [jnp.full((1, wide), 1.0) * pixels, jnp.zeros((4, wide), F32)], axis=0
    )
    usable, behind, ahead = (m[:, :frame_dev] for m in found)
    copies[1].wait()
    x = spec[0].astype(F32) * usable
    lane = iota((1, frame_dev), 1)
    row = iota((rows, 1), 0)
    inner = jnp.where((lane > 0) & (lane < frame_dev - 1), usable, 0.0)
    number = (rows - 2) * jnp.sum(inner, axis=1, keepdims=True)
    inner = inner * ((row > 0) & (row < rows - 1)).astype(F32)
    centre = jnp.sum(jnp.sum(x, axis=0, keepdims=True), axis=1, keepdims=True)
    centre = centre / (rows * jnp.maximum(jnp.sum(usable, axis=1, keepdims=True), 1.0))
    centre = lax.reduce_precision(centre, 8, 7)
    shifted = [pltpu.roll(x, 1, 1) * behind, x, pltpu.roll(x, frame_dev - 1, 1) * ahead]
    taps = [pltpu.roll(v, (1 - i) % rows, 0) if i != 1 else v for i in range(3) for v in shifted]
    features = feature_rows(centre, (taps, inner))
    lane = iota((1, 128), 1)
    features = jnp.where(lane == 90, centre, jnp.where(lane == 91, number, features))
    pick = iota((8, frame_dev), 0)
    column = jnp.where(pick < 4, pick, frame_dev - 8 + pick)
    strip = dot((iota((8, frame_dev), 1) == column).astype(BF16), x.astype(BF16), ((1,), (1,)))
    lane = iota((8, 128), 1)
    repeat = (iota((rows, 128), 1) % rows == iota((rows, 128), 0)).astype(BF16)
    strip = jnp.where(lane // rows == iota((8, 128), 0), dot(strip.astype(BF16), repeat), 0.0)
    strip = jnp.sum(strip, axis=0, keepdims=True)

    def put(n, value):
        rows_out[pl.ds(n, devices, stride=FIRST), :] = jnp.broadcast_to(value, (devices, 128))

    near = jnp.concatenate([x[0:2], x[rows - 2 :]], axis=0)
    near = jnp.concatenate([near[:, :128], near[:, 128:]], axis=0)
    for d in range(devices):
        rows_out[FIRST * d : FIRST * d + 8, :] = near
    put(COLUMNS, strip)
    copies[2].wait()
    _, chan, many, half = own.shape
    share = share_of(devices, chan)
    holders = chan // share
    g = own[0].astype(F32)
    edges[0:chan] = g[:, 0, :]
    edges[chan:] = g[:, many - 1, :]

    def spread_out(v, held):
        if held < devices:
            v = jnp.concatenate([v, jnp.zeros((devices - held, 128), F32)], axis=0)
        return v

    for n in range(share):
        put(EDGES + n, spread_out(edges[n * holders : (n + 1) * holders, :], holders))
        put(EDGES + share + n, spread_out(edges[chan + n * holders : chan + (n + 1) * holders, :], holders))
    for n in range(2 * share, COLUMNS - EDGES):
        put(EDGES + n, jnp.zeros((1, 128), F32))
    end = iota((8, half), 0)
    at = iota((8, half), 1)
    ends = ((end == 0) & (at == 0)) | ((end == 1) & (at == half - 1))
    columns = dot(ends.astype(BF16), g.reshape(chan * many, half).astype(BF16), ((1,), (1,)))
    group = 128 // many
    source = iota((128, 128), 0)
    lane = iota((group, 128), 1)
    mine = lane // many == iota((group, 128), 0)
    lane8, own8 = iota((8, 128), 1), iota((8, 128), 0)
    parts = three_parts(features)
    for n in range(2):
        side = jnp.zeros((holders, 128), F32)
        for m in range(share):
            move = (iota((128, 128), 1) == SIDE + many * m + source % many).astype(BF16)
            first = m * holders * many // 128
            block = [columns[n : n + 1, 128 * q : 128 * (q + 1)] for q in range(first, first + holders * many // 128)]
            block = jnp.concatenate([jnp.where(mine, v, 0.0) for v in block], axis=0)
            side = side + dot(block.astype(BF16), move)
        far = x[2:4] if n == 0 else x[rows - 4 : rows - 2]
        pieces = [far[r : r + 1, 128 * h : 128 * (h + 1)] for r in range(2) for h in range(2)]
        pieces = jnp.concatenate([jnp.where(lane8 // 16 == own8, v, 0.0) for v in pieces], axis=0)
        far = dot(pieces.astype(BF16), (iota((128, 128), 1) == FAR + source % 16).astype(BF16))
        put(SUMS + n, spread_out(side, holders) + spread_out(far, FAR_HOLDERS) + parts[n])
    put(SUMS + 2, parts[2])
    out[...] = rows_out[...].reshape(out.shape).astype(BF16)


def weights(own, bounds_hbm, k2_hbm, k1_hbm, gain_one_hbm, bias_one_hbm, gain_two_hbm, bias_two_hbm,
            wf, wb, w1, ws_hbm, pairs, singles, k1t, params, all_masks, edge_masks, twice, own_rows,
            k2, k1, vectors, bounds, ws, temp, sems):
    loads = start_all(
        (bounds_hbm, bounds),
        (k2_hbm, k2),
        (k1_hbm, k1),
        (gain_one_hbm, vectors.at[0]),
        (bias_one_hbm, vectors.at[1]),
        (gain_two_hbm, vectors.at[2]),
        (bias_two_hbm, vectors.at[3]),
        sems=sems,
    )
    _, many, count, half = own.shape
    temp[...] = own[0].astype(F32).reshape(many * count, half)
    for r in range(count):
        own_rows[r * many : (r + 1) * many] = temp[pl.ds(r, many, stride=count), :].astype(BF16)
    wait_all(loads)
    chan = k2.shape[1]
    span = wf.shape[1]
    taps = [k2[t].astype(F32) for t in range(9)]
    rest = jnp.zeros((chan, span - 9 * chan), F32)
    forward = jnp.concatenate(taps + [rest], axis=1)
    backward = jnp.concatenate([taps[8 - t].T for t in range(9)] + [rest], axis=1)
    for r in range(wb.shape[0] // chan):
        at = slice(r * chan, (r + 1) * chan)
        wb[at] = (pltpu.roll(backward, 3 * chan * r, 1) if r else backward).astype(BF16)
    full = jnp.concatenate([k1[n].astype(F32) for n in range(3)] + [jnp.zeros((7, chan), F32)], axis=0)
    low = [
        jnp.concatenate([full[3 * (2 - a) + 2 - b : 3 * (2 - a) + 3 - b] for a in range(3)], axis=1)
        for b in range(3)
    ]
    rest = jnp.zeros((1, ws.shape[1] - 3 * chan), F32)
    for b in range(3):
        base = jnp.concatenate([low[b], rest], axis=1)
        many = ws.shape[0] // 3
        rolled = [pltpu.roll(base, chan * m, 1) if m else base for m in range(many)]
        ws[many * b : many * (b + 1)] = jnp.concatenate(rolled, axis=0).astype(BF16)
    store_ws = pltpu.make_async_copy(ws, ws_hbm, sems.at[7])
    store_ws.start()
    count, frame_dev = all_masks.shape[0] // 3, all_masks.shape[1]
    frames = iota((count, frame_dev), 0) * frame_dev + iota((count, frame_dev), 1)
    for n, mask in enumerate(frame_masks(bounds[...], frames)):
        all_masks[n * count : (n + 1) * count] = mask
    q = iota(edge_masks.shape, 0)
    lane = iota(edge_masks.shape, 1)
    k = q % 8
    frames = (q // 8) * frame_dev + jnp.where(k < 4, k, k + frame_dev - 8)
    living, behind, ahead = frame_masks(bounds[...], frames)
    living = jnp.where((k == 0) | (k == 7), living, 0.0)
    edge_masks[...] = jnp.where(lane == 0, living, jnp.where(lane == 1, behind, jnp.where(lane == 2, ahead, 0.0)))
    params[...] = jnp.concatenate(
        [vectors[n] for n in range(4)] + [jnp.zeros((4, chan), F32)], axis=0
    )
    tap = iota((16, 128), 0)
    lane = iota((16, 128), 1)
    i = (tap * 11) >> 5
    ninth = (lane * 57) >> 9
    to_band = (lane == BAND * (tap - 3 * i) + i) & (tap < 9)
    to_left = (ninth == tap) & (tap < 9)
    to_right = (lane - 9 * ninth == tap) & (lane < 81)
    to_single = (lane == 81 + tap) & (tap < 9)
    source = iota((128, 128), 0) - 81
    lane = iota((128, 128), 1)
    ninth = (lane * 57) >> 9
    inside = (source >= 0) & (source < 9) & (lane < 81)
    twice[...] = jnp.where(inside, (source == ninth).astype(F32) + (source == lane - 9 * ninth).astype(F32), 0.0)
    for r in range(wf.shape[0] // chan):
        at = slice(r * chan, (r + 1) * chan)
        wf[at] = (pltpu.roll(forward, 3 * chan * r, 1) if r else forward).astype(BF16)
    k1t[...] = full
    k = full.astype(BF16)
    lanes = [dot(k, select.astype(BF16), ((0,), (0,))) for select in (to_band, to_left, to_right, to_single)]
    pairs[...] = lanes[1] * lanes[2]
    singles[...] = lanes[3]
    for m in range(w1.shape[0] // chan):
        w1[m * chan : (m + 1) * chan] = (pltpu.roll(lanes[0], m, 1) if m else lanes[0]).astype(BF16)
    store_ws.wait()


def feature_rows(centre, *parts):
    def folded(v):
        return jnp.sum(halves(v), axis=0, keepdims=True)

    rows = [jnp.zeros((1, 128), F32)] * 96
    for taps, weight in parts:
        z = [tap - centre for tap in taps]
        for s in range(9):
            left = z[s] * weight
            rows[81 + s] = rows[81 + s] + folded(left)
            for t in range(s, 9):
                rows[9 * s + t] = rows[9 * t + s] = rows[9 * s + t] + folded(left * z[t])
    return to_lanes(jnp.sum(jnp.concatenate(rows, axis=0), axis=1, keepdims=True))


def summed_blocks(ref, devices, by=1):
    block = ref.shape[0] // devices
    period = max(8 // math.gcd(block, 8), by)
    step = period * block
    total = ref[0:step, :]
    for at in range(step, ref.shape[0], step):
        total = total + ref[at : at + step, :]
    results = []
    for first in range(by):
        result = total[first * block : (first + 1) * block]
        for n in range(first + by, period, by):
            result = result + total[n * block : (n + 1) * block]
        results.append(result)
    return results if by > 1 else results[0]


def moved_rows(v, step):
    if step == 0:
        return v
    count = v.shape[0]
    if abs(step) >= count:
        return jnp.zeros_like(v)
    zero = jnp.zeros((abs(step), v.shape[1]), v.dtype)
    if step > 0:
        return jnp.concatenate([zero, v[: count - step]], axis=0)
    return jnp.concatenate([v[-step:], zero], axis=0)


def silu_halves(h):
    t = jnp.tanh(h)
    one = 1.0 + t
    return h * one, one * (1.0 + h * (1.0 - t))


def act_row(act, r, low, low_masks):
    low = low * low_masks[0]
    chan = low.shape[0]
    for n, v in enumerate((low,) + shifted_frames(low, *low_masks[1:])):
        at = (3 * r + (1, 0, 2)[n]) * chan
        act[at : at + chan, :] = v


def forward_one(recv, spec, pairs, singles, twice, w1, wf, params, masks, all_masks, edge_masks,
                pre_two, payload, act, x3, far_rim, stats, features_out, pre_one, got, strips, halo, rows_out):
    devices = recv.shape[0]
    n_mel, count = lax.axis_size("mel"), lax.axis_size("tm")
    rows = MEL_ROWS
    mels = n_mel * rows
    wide = masks.shape[1]
    frame_dev = wide - RIM
    chan = params.shape[1]
    me_m, me_t = lax.axis_index("mel"), lax.axis_index("tm")
    usable, behind, ahead = (masks[n : n + 1] for n in range(3))
    total = masks[3:4, 0:1]
    got[...] = recv[...].astype(F32).reshape(devices * FIRST, 128)

    def every(n):
        return got[pl.ds(n, devices, stride=FIRST), :]

    lane = iota((count, 128), 1)
    bands = [got[pl.ds(FIRST * k * count + COLUMNS, count, stride=FIRST), :] for k in range(n_mel)]
    for c in range(8):
        column = jnp.zeros((count, 128), F32)
        for k, band in enumerate(bands):
            part = jnp.where(lane // rows == c, band, 0.0)
            column = column + (pltpu.roll(part, rows * (k - c) % 128, 1) if k != c else part)
        strips[pl.ds(c, count, stride=8), :] = column
    at = pl.multiple_of(FIRST * (jnp.maximum(me_m - 1, 0) * count + me_t), 8)
    above = got[pl.ds(at, 8), :] * (me_m > 0).astype(F32)
    at = pl.multiple_of(FIRST * (jnp.minimum(me_m + 1, n_mel - 1) * count + me_t), 8)
    below = got[pl.ds(at, 8), :] * (me_m < n_mel - 1).astype(F32)
    above = jnp.concatenate([above[2:4], above[6:8]], axis=1)
    below = jnp.concatenate([below[0:2], below[4:6]], axis=1)
    own = spec[0].astype(F32) * usable[:, :frame_dev]
    at = pl.multiple_of(8 * jnp.minimum(me_t + 1, count - 1), 8)
    after = strips[pl.ds(at, 8), :][:, :mels] * (me_t + 1 < count).astype(F32)
    at = pl.multiple_of(8 * jnp.maximum(me_t - 1, 0), 8)
    before = strips[pl.ds(at, 8), :][:, :mels] * (me_t > 0).astype(F32)
    sides = jnp.concatenate([after[0:4], before[4:8], jnp.zeros((8, mels), F32)], axis=0).astype(BF16)
    side = iota((16, RIM), 0)
    place = iota((16, RIM), 1) == jnp.where(side < 4, side, jnp.where(side < 8, side + RIM - 8, -1))
    halo[0:8] = jnp.zeros((8, RIM), F32)
    halo[mels : mels + 8] = jnp.zeros((8, RIM), F32)
    halo[4 : mels + 4] = dot(sides, place.astype(BF16), ((0,), (0,)))
    rim = halo[pl.ds(pl.multiple_of(me_m * rows, 8), BAND), :]
    far_rim[...] = rim
    row = iota((BAND, RIM), 0)
    rim = jnp.where((row >= 2) & (row < BAND - 2), rim, 0.0)
    blank = jnp.zeros((2, frame_dev), F32)
    near = jnp.concatenate([jnp.concatenate([blank, above, own, below, blank], axis=0), rim], axis=1)
    x3[...] = jnp.concatenate(
        [
            pltpu.roll(near, 1, 1) * behind,
            near,
            pltpu.roll(near, wide - 1, 1) * ahead,
            jnp.broadcast_to(usable, (BAND, wide)),
            jnp.zeros((128 - 4 * BAND, wide), F32),
        ],
        axis=0,
    ).astype(BF16)
    pre_one[2 * chan : (rows + 4) * chan] = dot(w1[2 * chan : (rows + 4) * chan, :], x3[...])
    lane = iota((1, 128), 1)
    parts = jnp.where(lane < 92, every(SUMS) + every(SUMS + 1) + every(SUMS + 2), 0.0)
    centres, numbers = parts[:, 90:91], parts[:, 91:92]
    centre = jnp.sum(centres * numbers, axis=0, keepdims=True)
    centre = centre / jnp.maximum(jnp.sum(numbers, axis=0, keepdims=True), 1.0)
    delta = centres - centre
    features = jnp.sum(parts + delta * numbers * jnp.where(lane < 81, delta, 1.0), axis=0, keepdims=True)
    moved = jnp.sum(delta * parts, axis=0, keepdims=True)
    def edge_row(k, n):
        first = FIRST * k * count + n
        return jnp.concatenate(
            [got[pl.ds(first, count, stride=FIRST), :], got[pl.ds(first + 4, count, stride=FIRST), :]], axis=1
        )

    edge_rows = [[edge_row(k, n) for n in range(4)] for k in range(n_mel)]
    zero = jnp.zeros((count, frame_dev), F32)
    rows_of = [[], [], []]
    for k, (top, second, fore, bottom) in enumerate(edge_rows):
        for n, v in enumerate((edge_rows[k - 1][3] if k else zero, top, second)):
            rows_of[n].append(v)
        for n, v in enumerate((fore, bottom, edge_rows[k + 1][0] if k + 1 < n_mel else zero)):
            rows_of[n].append(v)
    f_usable, f_behind, f_ahead = (all_masks[n * count : (n + 1) * count, :] for n in range(3))
    lane = iota((count, frame_dev), 1)

    def frame_before(v):
        v = pltpu.roll(v, 1, 1)
        return jnp.where(lane == 0, pltpu.roll(v, 1, 0), v) * f_behind

    def frame_after(v):
        v = pltpu.roll(v, frame_dev - 1, 1)
        return jnp.where(lane == frame_dev - 1, pltpu.roll(v, count - 1, 0), v) * f_ahead

    taps = []
    for group in rows_of:
        for move in (frame_before, lambda v: v, frame_after):
            taps.append(jnp.concatenate([move(v) for v in group], axis=1))
    f_usable = jnp.concatenate([f_usable] * (2 * n_mel), axis=1)
    borders = (taps, f_usable)
    edge = strips[...]
    q_usable, q_behind, q_ahead = (edge_masks[:, n : n + 1] for n in range(3))
    lane = iota((count * 8, 128), 1)
    inside = (lane < mels) & (lane % rows != 0) & (lane % rows != rows - 1)
    shifted = [
        pltpu.roll(edge, 1, 0) * q_behind,
        edge,
        pltpu.roll(edge, count * 8 - 1, 0) * q_ahead,
    ]
    taps = [pltpu.roll(v, (1 - i) % 128, 1) if i != 1 else v for i in range(3) for v in shifted]
    features = features + feature_rows(centre, borders, (taps, jnp.where(inside, q_usable, 0.0)))
    features = jnp.where(iota((1, 128), 1) < 90, features, 0.0)
    near_mean = jnp.sum(singles[...] * features, axis=1, keepdims=True) / total
    around = jnp.sum(singles[...], axis=1, keepdims=True)
    square = jnp.sum(pairs[...] * features, axis=1, keepdims=True)
    square = (square + 2.0 * around * jnp.sum(singles[...] * moved, axis=1, keepdims=True)) / total
    inv = lax.rsqrt(square - near_mean * near_mean + 1e-05)
    mean = near_mean + centre * around
    lane = iota((chan, 128), 1)
    stats[0:chan] = jnp.where(lane == 0, mean, jnp.where(lane == 1, inv, 0.0))
    stats[chan : chan + 8] = jnp.broadcast_to(to_lanes(near_mean), (8, 128))
    stats[chan + 8 : chan + 16] = jnp.broadcast_to(to_lanes(inv), (8, 128))
    scale = 0.5 * to_column(params[0:1], chan) * inv
    shift = 0.5 * to_column(params[1:2], chan) - mean * scale
    stats[chan + 16 :] = jnp.where(lane == 0, scale, jnp.where(lane == 1, shift, 0.0))
    scale = jnp.broadcast_to(scale, (chan, wide))
    shift = jnp.broadcast_to(shift, (chan, wide))
    block, taps = wf.shape
    first = jnp.zeros((chan, 128), F32)
    second = jnp.zeros((chan, 128), F32)
    own_mask = usable[:, :frame_dev]
    low_masks = [m.astype(BF16) for m in (usable, behind, ahead)]
    for r in range(2, rows + 4):
        value, _ = silu_halves(pre_one[r * chan : (r + 1) * chan, :] * scale + shift)
        if not 0 <= r - 3 < rows:
            value = value * row_valid(r - 3, rows)
        act_row(act, r, value.astype(BF16), low_masks)
        if r < 5 or r % 2 == 0:
            continue
        g = (r - 3) // 2
        result = dot(wf[...], act[g * 3 * block : g * 3 * block + taps, :frame_dev])
        at = (g - 1) * block
        pre_two[at : at + block, :frame_dev] = result
        if g % 2 == 0:
            beside = [act[n * 3 * block : n * 3 * block + taps, frame_dev:] for n in (g - 1, g)]
            beside = dot(wf[...], jnp.concatenate(beside, axis=1))
            for n in range(2):
                pre_two[at + (n - 1) * block : at + n * block, frame_dev:] = beside[:, n * RIM : (n + 1) * RIM]
        for q in range(2):
            p = result[q * chan : (q + 1) * chan]
            masked = p * own_mask
            first = first + halves(masked)
            second = second + halves(masked * p)
    moved = dot(jnp.broadcast_to(moved, (8, 128)), twice[...], precision=EXACT)[0:1]
    features_out[...] = jnp.concatenate(
        [features + moved, jnp.broadcast_to(centre, (1, 128)), jnp.zeros((6, 128), F32)], axis=0
    )
    share = share_of(devices, chan)

    def put(n, value):
        rows_out[pl.ds(n, devices, stride=SECOND), :] = jnp.broadcast_to(value, (devices, 128))

    for n in range(share):
        put(3 + n, moved_rows(every(EDGES + share + n), count))
        put(3 + share + n, moved_rows(every(EDGES + n), -count))
    for n in [0, 1, 2] + list(range(3 + 2 * share, SECOND - 1)):
        put(n, jnp.zeros((1, 128), F32))
    lane = iota((devices, 128), 1)
    tm = iota((devices, 128), 0) % count
    at_side = (lane >= SIDE) & (lane < FAR)
    lefts = jnp.where(at_side, every(SUMS), 0.0)
    rights = jnp.where(at_side, every(SUMS + 1), 0.0)
    beside = jnp.zeros((devices, 128), F32)
    for n, step in enumerate((0, count, -count)):
        one = jnp.where(tm > 0, moved_rows(rights, step + 1), 0.0)
        two = jnp.where(tm < count - 1, moved_rows(lefts, step - 1), 0.0)
        beside = beside + pltpu.roll(one, (32 * n - SIDE) % 128, 1) + pltpu.roll(two, (32 * n + 16 - SIDE) % 128, 1)
    outer = jnp.where(lane >= FAR, moved_rows(every(SUMS + 1), count), 0.0)
    beside = beside + pltpu.roll(outer, 128 - 16, 1)
    beside = beside + jnp.where(lane >= FAR, moved_rows(every(SUMS), -count), 0.0)
    put(SECOND - 1, beside)
    first = jnp.sum(first, axis=1, keepdims=True)
    second = jnp.sum(second, axis=1, keepdims=True)
    parts = list(three_parts(to_lanes(first) + to_lanes(second, chan)))
    parts = jnp.concatenate(parts + [jnp.zeros((SECOND - 3, 128), F32)], axis=0)
    for d in range(devices):
        payload[d] = (rows_out[SECOND * d : SECOND * (d + 1), :] + parts).astype(BF16)


def spreading(half):
    lane = iota((half, 2 * half), 1)
    return jnp.where(lane >> 1 == iota((half, 2 * half), 0), 0.25, 0.0).astype(BF16)


def half_share(devices, taps):
    return -(-taps // 2 // devices)


def backward_scaled(recv, pre_two, act, own_rows, params, masks,
                    grad, kept_half, sent_half, totals, stats, pairs, up, right, halved):
    devices = recv.shape[0]
    chan = params.shape[1]
    half = own_rows.shape[1]
    frame_dev = 2 * half
    rows = MEL_ROWS
    up[...] = dot(own_rows[...], spreading(half))
    usable = masks[0:1, :frame_dev]
    total = masks[3:4, 0:1]
    sums = [recv[d].astype(F32) for d in range(devices)]
    while len(sums) > 1:
        sums = [a + b for a, b in zip(sums[0::2], sums[1::2])]
    sums = jnp.sum(sums[0][0:3], axis=0, keepdims=True)
    mean = to_column(sums, chan) / total
    inv = lax.rsqrt(to_column(sums, chan, chan) / total - mean * mean + 1e-05)
    scale = 0.5 * to_column(params[2:3], chan) * inv
    shift = 0.5 * to_column(params[3:4], chan) - mean * scale
    lane = iota((chan, 128), 1)
    columns = jnp.zeros((chan, 128), F32)
    for n, column in enumerate((mean, inv, scale, shift)):
        columns = jnp.where(lane == n, column, columns)
    stats[0:chan] = columns
    stats[chan : chan + 8] = jnp.broadcast_to(to_lanes(inv), (8, 128))
    mean, inv, scale, shift = (jnp.broadcast_to(v, (chan, frame_dev)) for v in (mean, inv, scale, shift))
    first = jnp.zeros((chan, 128), F32)
    second = jnp.zeros((chan, 128), F32)
    mask = 0.5 * usable
    right[3 * chan :] = jnp.ones((16, rows * frame_dev), BF16)
    table = jnp.zeros((9 * chan, 3 * chan + 16), F32)
    for m in range(rows):
        at = slice(m * chan, (m + 1) * chan)
        pre = pre_two[at, :frame_dev]
        value, slope = silu_halves(pre * scale + shift)
        value = value * usable
        both = value if m % 2 == 0 else both + value
        if m % 2:
            pairs[m // 2 * chan : (m // 2 + 1) * chan, :] = both
        g = up[m // 2 * chan : (m // 2 + 1) * chan, :] * slope * mask
        grad[at, :] = g
        normed = (pre - mean) * inv
        first = first + halves(g * normed)
        second = second + halves(g)
        lanes = slice(m * frame_dev, (m + 1) * frame_dev)
        right[0:chan, lanes] = g.astype(BF16)
        right[chan : 2 * chan, lanes] = normed.astype(BF16)
        right[2 * chan : 3 * chan, lanes] = (g - right[0:chan, lanes].astype(F32)).astype(BF16)
        if m in (5, 11, rows - 1):
            start = m - m % 6
            left = [act[(n + 2) * 3 * chan : (n + 5) * 3 * chan, :frame_dev] for n in range(start, m + 1)]
            lanes = slice(start * frame_dev, (m + 1) * frame_dev)
            table = table + dot(jnp.concatenate(left, axis=1), right[:, lanes], ((1,), (1,)))
    first = jnp.sum(first, axis=1, keepdims=True)
    second = jnp.sum(second, axis=1, keepdims=True)
    totals[...] = jnp.broadcast_to(to_lanes(first) + to_lanes(second, chan), (8, 128))
    rest = jnp.concatenate([table[:, 2 * chan :], jnp.zeros((9 * chan, chan - 16), F32)], axis=1)
    both = table[:, : 2 * chan] + jnp.where(iota(rest.shape, 1) < chan, rest, 0.0)
    single = rest[:, chan : chan + 1]
    taps = 9 * chan // 2
    lane = iota((devices, 128), 1)
    for h in range(2):
        halved[h, 0:taps] = both[h * taps : (h + 1) * taps]
        constants = jnp.zeros((devices, 128), F32)
        for k in range(half_share(devices, 9 * chan)):
            at = h * taps + k * devices
            ones = single[at : min(at + devices, (h + 1) * taps)]
            if ones.shape[0] < devices:
                ones = jnp.concatenate([ones, jnp.zeros((devices - ones.shape[0], 1), F32)], axis=0)
            constants = jnp.where(lane == k, ones, constants)
        halved[h, taps:] = constants
    core = lax.axis_index("tm") % 2
    kept_half[...] = halved[core]
    sent_half[...] = halved[1 - core]


def around(recv, pre_two, act, w1, wf, x3, far_rim, stats_one, masks, stats, pre_ring, ring, rim,
           sides, up, got, beyond, more):
    devices = recv.shape[0]
    got[...] = recv[:, 0:SECOND, :].astype(F32).reshape(devices * SECOND, 128)
    rows = MEL_ROWS
    many = rows // 2
    wide = pre_two.shape[1]
    frame_dev = wide - RIM
    chan = pre_two.shape[0] // rows
    usable = masks[0:1]
    low_masks = [masks[n : n + 1].astype(BF16) for n in range(3)]
    pieces = got[pl.ds(SECOND - 1, devices, stride=SECOND), :][:FAR_HOLDERS].astype(BF16)
    source = iota((128, 128), 0)
    lane = iota((FAR_HOLDERS, 128), 1)
    mine = lane // 16 == iota((FAR_HOLDERS, 128), 0) % 8
    outer = []
    for first in (SIDE, FAR):
        place = (source - first == iota((128, 128), 1) % 16).astype(BF16)
        v = jnp.where(mine, dot(pieces, place), 0.0)
        v = [jnp.sum(v[8 * n : 8 * n + 8], axis=0, keepdims=True) for n in range(4)]
        outer += [jnp.concatenate(v[2 * r : 2 * r + 2], axis=1) for r in range(2)]
    blank = jnp.zeros((BAND - 4, frame_dev), F32)
    far = jnp.concatenate(outer[:2] + [blank] + outer[2:], axis=0)
    row = iota((BAND, RIM), 0)
    far = jnp.concatenate([far, jnp.where((row < 2) | (row >= BAND - 2), far_rim[...], 0.0)], axis=1)
    far = jnp.concatenate(
        [
            pltpu.roll(far, 1, 1) * masks[1:2],
            far,
            pltpu.roll(far, wide - 1, 1) * masks[2:3],
            jnp.zeros((128 - 3 * BAND, wide), F32),
        ],
        axis=0,
    )
    x_all = (x3[...].astype(F32) + far).astype(BF16)
    scale = jnp.broadcast_to(stats_one[chan + 16 :, 0:1], (chan, wide))
    shift = jnp.broadcast_to(stats_one[chan + 16 :, 1:2], (chan, wide))
    for h, start in enumerate((0, rows + 4)):
        pre_one = dot(w1[start * chan : (start + 2) * chan, :], x_all)
        for n in range(2):
            value, _ = silu_halves(pre_one[n * chan : (n + 1) * chan] * scale + shift)
            value = value * row_valid(start + n - 3, rows)
            act_row(more, 2 * h + n, value.astype(BF16), low_masks)
    line = 3 * chan
    above = jnp.concatenate([more[0 : 2 * line, :], act[2 * line : 4 * line, :]], axis=0)
    below = jnp.concatenate([act[(rows + 2) * line : (rows + 4) * line, :], more[2 * line :, :]], axis=0)
    pre_ring[0 : 2 * chan] = dot(wf[...], above)
    pre_ring[2 * chan :] = dot(wf[...], below)
    share = share_of(devices, chan)
    holders = chan // share

    def every(n):
        return got[pl.ds(n, devices, stride=SECOND), :]

    beside = 0.25 * every(SECOND - 1)[:holders]
    lane = iota((holders, RIM), 1)
    for n in range(share):
        first = n * holders
        beyond[first : first + holders, :] = every(3 + n)[:holders]
        beyond[chan + first : chan + first + holders, :] = every(3 + share + n)[:holders]
        for r in range(many + 2):
            at = many * n + (r if r < many else 32 + many - 1 if r == many else 64)
            left, right_of = beside[:, at : at + 1], beside[:, at + 16 : at + 17]
            side = jnp.where(lane >= RIM - 2, left, jnp.where(lane < 2, right_of, 0.0))
            sides[r * chan + first : r * chan + first + holders, :] = side
    up[...] = dot(beyond[...].astype(BF16), spreading(frame_dev // 2))
    scale = jnp.broadcast_to(stats[0:chan, 2:3], (chan, wide))
    shift = jnp.broadcast_to(stats[0:chan, 3:4], (chan, wide))
    for n, m in enumerate((-2, -1, rows, rows + 1)):
        below = n // 2
        upstream = jnp.concatenate(
            [
                up[below * chan : (below + 1) * chan, :],
                sides[(many + below) * chan : (many + below + 1) * chan, :],
            ],
            axis=1,
        )
        _, slope = silu_halves(pre_ring[n * chan : (n + 1) * chan, :] * scale + shift)
        ring[n * chan : (n + 1) * chan, :] = upstream * slope * (usable * (0.5 * row_valid(m, rows)))
    for m in range(rows):
        at = slice(m * chan, (m + 1) * chan)
        _, slope = silu_halves(pre_two[at, frame_dev:] * scale[:, frame_dev:] + shift[:, frame_dev:])
        upstream = sides[m // 2 * chan : (m // 2 + 1) * chan, :]
        rim[m * chan : (m + 1) * chan, :] = upstream * slope * (0.5 * usable[:, frame_dev:])


def pack_sums(kept_half, received, totals, after, payload):
    del after
    devices = kept_half.shape[0] - TAPS // 2
    block = payload.shape[0] // devices
    payload[pl.ds(0, devices, stride=block), :] = jnp.broadcast_to(totals[0:1], (devices, 128))
    taps = TAPS // 2
    total = kept_half[...] + received[...]
    for k in range(block - 2):
        cut = total[k * devices : min((k + 1) * devices, taps)]
        if cut.shape[0] < devices:
            cut = jnp.concatenate([cut, jnp.zeros((devices - cut.shape[0], 128), F32)], axis=0)
        payload[pl.ds(1 + k, devices, stride=block), :] = cut
    payload[pl.ds(block - 1, devices, stride=block), :] = total[taps:]


def pool(totals, pairs, out, gain_out, bias_out, temp):
    gain_out[...] = totals[0:1, : gain_out.shape[1]]
    bias_out[...] = totals[0:1, gain_out.shape[1] :]
    chan, rows, half = out.shape[1:]
    to_mean = jnp.where(iota((2 * half, half), 0) >> 1 == iota((2 * half, half), 1), 0.25, 0.0)
    pooled = dot(pairs[...], to_mean, precision=EXACT)
    for r in range(rows):
        temp[pl.ds(r, chan, stride=rows), :] = pooled[r * chan : (r + 1) * chan]
    out[0] = temp[...].reshape(chan, rows, half).astype(BF16)


def backward(recv, pre_two, pre_ring, grad, ring, rim, stats_two, w1, x3, stats, params, masks, wb,
             out, own_low, payload, totals, g3, pre_one, g1):
    chan = params.shape[1]
    rows = MEL_ROWS
    wide = pre_two.shape[1]
    frame_dev = wide - RIM
    usable = masks[0:1]
    behind, ahead = (masks[n : n + 1].astype(BF16) for n in (1, 2))
    total = masks[3:4, 0:1]
    devices = payload.shape[0]
    pre_one[...] = dot(w1[3 * chan : (rows + 3) * chan], x3[:, :frame_dev])

    even, odd = summed_blocks(recv, devices, 2)
    sums = even[0:1] + odd[0:1]
    gain_sum, bias_sum = sums[:, :chan], sums[:, chan:]
    totals[...] = jnp.broadcast_to(sums, (8, 128))
    mean, inv = stats_two[0:chan, 0:1], stats_two[0:chan, 1:2]
    factor = to_column(params[2:3], chan) * inv
    gain_part = factor * (to_column(sums, chan) / total * inv)
    bias_part = factor * (to_column(sums, chan, chan) / total) - mean * gain_part
    gain_part = jnp.broadcast_to(gain_part, (chan, wide))
    bias_part = jnp.broadcast_to(bias_part, (chan, wide))
    factor = jnp.broadcast_to(factor, (chan, wide))
    scale = jnp.broadcast_to(stats[chan + 16 :, 0:1], (chan, frame_dev))
    shift = jnp.broadcast_to(stats[chan + 16 :, 1:2], (chan, frame_dev))
    factor_one = jnp.broadcast_to(to_column(params[0:1], chan) * stats[0:chan, 1:2], (chan, frame_dev))
    own_mask = 0.5 * usable[:, :frame_dev]
    count = rows + 4
    share = even.shape[0] - 2
    mine = jnp.concatenate([even[1 : share + 1], odd[1 : share + 1]], axis=0)
    single = jnp.concatenate([to_column(v[share + 1 :], share) for v in (even, odd)], axis=0)
    factor_l = params[2:3] * stats_two[chan : chan + 1, :chan]
    mine = mine[:, :chan] - (bias_sum * single + gain_sum * mine[:, chan:]) / total
    mine = factor_l * mine
    mine = jnp.concatenate([mine[:share], mine[share:]], axis=1)
    if share < 9:
        mine = jnp.concatenate([mine, jnp.zeros((9 - share, 128), F32)], axis=0)
    table = jnp.zeros((chan, 128), F32)

    def tap_sums(m):
        taps_in = jnp.concatenate([x3[:, :frame_dev]] * 2, axis=1)
        products = dot(g1[m * chan : (m + 4) * chan, :], taps_in, ((1,), (1,)))
        moved = [pltpu.roll(products[k * chan : (k + 1) * chan], 128 - (m + k + 3), 1) for k in range(4)]
        return (moved[0] + moved[1]) + (moved[2] + moved[3])

    for q in range(count):
        at = slice(q * chan, (q + 1) * chan)
        mask = usable if 0 <= q - 2 < rows else usable * row_valid(q - 2, rows)
        if 2 <= q < rows + 2:
            own = slice((q - 2) * chan, (q - 1) * chan)
            pre, scaled = pre_two[own, :], jnp.concatenate([grad[own, :], rim[own, :]], axis=1)
        else:
            n = q if q < 2 else q - rows
            pre, scaled = pre_ring[n * chan : (n + 1) * chan, :], ring[n * chan : (n + 1) * chan, :]
        low = (factor * scaled - (bias_part + pre * gain_part) * mask).astype(BF16)
        out[at, :] = low
        if not 1 <= q < count - 1:
            continue
        base = (q - 1) * 3 * chan
        for n, v in enumerate((low,) + shifted_frames(low, behind, ahead)):
            spot = base + (1, 0, 2)[n] * chan
            g3[spot : spot + chan, :] = v[:, :frame_dev]
        start = q - 4
        if start < 0 or start % 2:
            continue
        result = dot(wb[...], g3[start * 3 * chan : (start + 4) * 3 * chan, :])
        for n in range(2):
            m = start + n
            at = slice(m * chan, (m + 1) * chan)
            _, slope = silu_halves(pre_one[at, :] * scale + shift)
            value = result[n * chan : (n + 1) * chan] * slope * own_mask
            own_low[at, :] = (value * factor_one).astype(BF16)
            g1[at, :frame_dev] = value.astype(BF16)
            g1[at, frame_dev:] = (value - g1[at, :frame_dev].astype(F32)).astype(BF16)
        if start % 4 == 2 and start > 2:
            table = table + tap_sums(start - 6)
    table = table + tap_sums(rows - 4)
    table = table.T
    places = [BAND * j + i for i in range(3) for j in range(3)] + [3 * BAND]
    rows10 = jnp.concatenate([table[n : n + 1] for n in places], axis=0)
    sums = jnp.concatenate([rows10[0:5], rows10[5:10]], axis=1)
    block = jnp.concatenate(list(three_parts(sums)) + [mine], axis=0).astype(BF16)
    for d in range(devices):
        payload[d] = block


def transposed(grad, own_low, w1, wb, x3, stats, features, k1t, params, masks, ws_hbm,
               first, ws, normed_taps, low, g3, rim, sem):
    load = pltpu.make_async_copy(ws_hbm, ws, sem)
    load.start()
    rows = MEL_ROWS
    chan = own_low.shape[0] // rows
    wide = grad.shape[1]
    frame_dev = wide - RIM
    count = grad.shape[0] // chan
    usable = masks[0:1]
    behind, ahead = (masks[n : n + 1].astype(BF16) for n in (1, 2))
    scale = jnp.broadcast_to(stats[chan + 16 :, 0:1], (chan, wide))
    shift = jnp.broadcast_to(stats[chan + 16 :, 1:2], (chan, wide))
    factor = jnp.broadcast_to(to_column(params[0:1], chan) * stats[0:chan, 1:2], (chan, wide))
    edge = (0, 1, 2, 3, count - 4, count - 3, count - 2, count - 1)
    for q in range(count):
        value = grad[q * chan : (q + 1) * chan, :]
        for n, v in enumerate((value,) + shifted_frames(value, behind, ahead)):
            spot = (3 * q + (1, 0, 2)[n]) * chan
            rim[spot : spot + chan, :] = v[:, frame_dev:]
            if q in edge:
                spot = (3 * edge.index(q) + (1, 0, 2)[n]) * chan
                g3[spot : spot + chan, :] = v[:, :frame_dev]
    low[chan : (rows + 1) * chan, :frame_dev] = own_low[...]

    def put(m, lanes, result, pre_one):
        at = slice((m + 1) * chan, (m + 2) * chan)
        _, slope = silu_halves(pre_one * scale[:, lanes] + shift[:, lanes])
        mask = usable[:, lanes] * (0.5 * row_valid(m, rows))
        low[at, lanes] = (result * slope * mask * factor[:, lanes]).astype(BF16)

    pre_one = dot(w1[2 * chan : (rows + 4) * chan, :], x3[:, frame_dev:])
    beside = slice(frame_dev, wide)
    for start in range(0, rows + 2, 2):
        result = dot(wb[...], rim[start * 3 * chan : (start + 4) * 3 * chan, :])
        for n in range(2):
            at = slice((start + n) * chan, (start + n + 1) * chan)
            put(start + n - 1, beside, result[n * chan : (n + 1) * chan], pre_one[at])
    own = slice(0, frame_dev)
    result = dot(wb[...], g3[: 4 * 3 * chan, :])
    put(-1, own, result[:chan], dot(w1[2 * chan : 3 * chan, :], x3[:, :frame_dev]))
    result = dot(wb[...], g3[4 * 3 * chan :, :])
    put(rows, own, result[chan:], dot(w1[(rows + 3) * chan : (rows + 4) * chan, :], x3[:, :frame_dev]))
    row = features[0:1, :]
    lane = iota((1, 128), 1)
    gram = jnp.concatenate(
        [jnp.where(lane < 9, pltpu.roll(row, 128 - 9 * t, 1) if t else row, 0.0) for t in range(9)]
        + [jnp.zeros((7, 128), F32)],
        axis=0,
    )
    single = to_column(row, 16, 81)[0:9]
    k_rows = jnp.concatenate([k1t[...], jnp.zeros((112, chan), F32)], axis=0)
    mean_l, inv_l = stats[chan : chan + 1, :chan], stats[chan + 8 : chan + 9, :chan]
    normed = inv_l * (dot(gram, k_rows, precision=EXACT)[0:9] - single * mean_l)
    normed_taps[0:16] = jnp.concatenate([normed, jnp.zeros((7, chan), F32)], axis=0)
    normed_taps[16:32] = jnp.broadcast_to(to_column(row, 16, 81), (16, chan))
    load.wait()
    first[...] = dot(ws[...], low[...])


def finish(recv, features, stats, k1t, first, ws, w1, x3, normed_taps, params, masks,
           spec_hbm, kernel_one_hbm, kernel_two_hbm, gain_hbm, bias_hbm,
           spec_grad, kernel_one, kernel_two, gain_out, bias_out, got, sems):
    chan = params.shape[1]
    rows = MEL_ROWS
    wide = x3.shape[1]
    frame_dev = wide - RIM
    usable, behind, ahead = (masks[n : n + 1] for n in range(3))
    total = masks[3:4, 0:1]
    gain = params[0:1]
    count = recv.shape[0]
    share = half_share(count, 9 * chan)
    got[...] = recv[...].astype(F32).reshape(count * LAST, 128)
    sums = summed_blocks(got, count)
    sums = sums[0:5] + sums[5:10] + sums[10:15]
    ten = jnp.concatenate([sums[:, :chan], sums[:, chan:]], axis=0)
    bias_sum = ten[9:10]
    mean_l, inv_l = stats[chan : chan + 1, :chan], stats[chan + 8 : chan + 9, :chan]
    ten = ten - features[1:2, 0:1] * bias_sum
    k = k1t[0:9]
    gain_sum = inv_l * (jnp.sum(k * ten[0:9], axis=0, keepdims=True) - mean_l * bias_sum)
    gain_out[...] = gain_sum
    bias_out[...] = bias_sum
    factor_l = gain * inv_l
    scale = factor_l * gain_sum / total * inv_l
    scale = jnp.concatenate(
        [scale * row_valid(-1, rows)] + [scale] * rows + [scale * row_valid(rows, rows)], axis=1
    )
    many = 3 * rows

    def in_parts(v, right):
        high = lax.reduce_precision(v, 8, 7)
        v = dot(jnp.concatenate([high, v - high], axis=0).astype(BF16), right)
        return v[:many] + v[many:]

    combined = in_parts(ws[...].astype(F32) * scale, w1[2 * chan : (rows + 4) * chan, :])
    left = [got[pl.ds(15 + p, count, stride=LAST), :] for p in range(share)]
    taps = TAPS // 2
    whole = [jnp.concatenate([v[:, h * chan : (h + 1) * chan] for v in left], axis=0)[:taps] for h in range(2)]
    whole = jnp.concatenate(whole, axis=0)
    for t in range(9):
        kernel_two[t] = whole[t * chan : (t + 1) * chan].T
    stores = [pltpu.make_async_copy(kernel_two, kernel_two_hbm, sems.at[4])]
    stores[0].start()
    taken = in_parts(combined, x3[...])
    taps = first[...] - taken
    moved = [taps[rows * b : rows * (b + 1)] for b in range(3)]
    mean_full = mean_l + features[1:2, 0:1] * jnp.sum(k, axis=0, keepdims=True)
    constant = jnp.sum(k * (factor_l * (bias_sum - gain_sum * inv_l * mean_full) / total), axis=1, keepdims=True)
    for a in range(3):
        row = iota((rows, 1), 0) + (a - 1) + lax.axis_index("mel") * rows
        valid = ((row >= 0) & (row < lax.axis_size("mel") * rows)).astype(F32) * usable
        for b in range(3):
            t = 3 * (2 - a) + 2 - b
            moved[b] = moved[b] - constant[t : t + 1] * valid
    result = pltpu.roll(moved[0], 1, 1) * behind + moved[1] + pltpu.roll(moved[2], wide - 1, 1) * ahead
    spec_grad[0] = (result * usable)[:, :frame_dev]
    grad_taps = factor_l * (ten[0:9] - (bias_sum * normed_taps[16:25] + gain_sum * normed_taps[0:9]) / total)
    for i in range(3):
        kernel_one[i] = grad_taps[3 * i : 3 * i + 3]
    outs = ((spec_grad, spec_hbm), (kernel_one, kernel_one_hbm), (gain_out, gain_hbm), (bias_out, bias_hbm))
    wait_all(stores + start_all(*outs, sems=sems))


def run(kernel, outs, scratch, *args, hbm=0, apart=(), flops=10**8, size=4 * 10**6):
    vmem = pl.BlockSpec(memory_space=pltpu.VMEM)
    devices = lax.axis_size("mel") * lax.axis_size("tm")
    specs = []
    args = list(args)
    for n, a in enumerate(args):
        if hbm and n >= len(args) - hbm:
            specs.append(pl.BlockSpec(memory_space=pltpu.HBM))
            args[n] = pltpu.with_memory_space_constraint(a, pltpu.HBM)
        else:
            specs.append(vmem)
            args[n] = pltpu.with_memory_space_constraint(a, pltpu.VMEM)
    return pl.pallas_call(
        kernel,
        out_shape=outs,
        in_specs=specs,
        out_specs=[pl.BlockSpec(memory_space=pltpu.HBM) if n in apart else vmem for n in range(len(outs))],
        scratch_shapes=scratch,
        compiler_params=pltpu.CompilerParams(vmem_limit_bytes=(29 + devices // 32) * 2**20),
        cost_estimate=pl.CostEstimate(flops=flops, bytes_accessed=size, transcendentals=0),
    )(*args)


def shape(dims, dtype=F32):
    return jax.ShapeDtypeStruct(dims, dtype)


def kept(dims, dtype=F32):
    return pltpu.VMEM(dims, dtype)


def far(dims, dtype=F32):
    return pltpu.HBM(dims, dtype)


def exchange(blocks, axes=AXES):
    return lax.all_to_all(blocks, axes, 0, 0, tiled=True)


def exchange_rows(rows, axes=AXES):
    return exchange(rows[:, None, :], axes)[:, 0, :]


def shards(spectrum, clip_bounds, kernel_one, gain_one, bias_one, kernel_two, gain_two, bias_two, pooled_grad):
    _, rows, frame_dev = spectrum.shape
    chan = kernel_two.shape[0]
    n_mel, n_tm = lax.axis_size("mel"), lax.axis_size("tm")
    devices = n_mel * n_tm
    half = frame_dev // 2
    wide = frame_dev + RIM
    mels = n_mel * rows

    packed, own, spec, masks = run(
        pack,
        [
            kept((devices, FIRST, 128), BF16),
            kept(pooled_grad.shape, BF16),
            kept(spectrum.shape, BF16),
            kept((8, wide)),
        ],
        [
            pltpu.VMEM(clip_bounds.shape, jnp.int32),
            pltpu.VMEM((2 * chan, half), F32),
            pltpu.VMEM((devices * FIRST, 128), F32),
            pltpu.SemaphoreType.DMA((3,)),
        ],
        spectrum,
        pooled_grad,
        clip_bounds,
        hbm=3,
    )
    recv = exchange(packed)
    ext = rows + 6
    span = 4 * 3 * chan
    wf, wb, w1, ws, pairs, singles, k1t, params, all_masks, edge_masks, twice, own_rows = run(
        weights,
        [
            kept((2 * chan, span), BF16),
            kept((2 * chan, span), BF16),
            kept((ext * chan, 128), BF16),
            far((rows * 3, (rows + 2) * chan), BF16),
            kept((chan, 128)),
            kept((chan, 128)),
            kept((16, chan)),
            kept((8, chan)),
            kept((3 * n_tm, frame_dev)),
            kept((n_tm * 8, 128)),
            kept((128, 128)),
            kept((chan * rows // 2, half), BF16),
        ],
        [
            pltpu.VMEM((9, chan, chan), BF16),
            pltpu.VMEM((3, 3, chan), BF16),
            pltpu.VMEM((4, 1, chan), F32),
            pltpu.VMEM(clip_bounds.shape, jnp.int32),
            pltpu.VMEM((rows * 3, (rows + 2) * chan), BF16),
            pltpu.VMEM((chan * rows // 2, half), F32),
            pltpu.SemaphoreType.DMA((8,)),
        ],
        own,
        clip_bounds,
        jnp.transpose(kernel_two, (2, 3, 0, 1)).reshape(9, chan, chan),
        jnp.transpose(kernel_one, (1, 2, 0)),
        gain_one[None],
        bias_one[None],
        gain_two[None],
        bias_two[None],
        hbm=7,
        apart=(3,),
    )
    pre_two, payload, act, x3, far_rim, stats_one, features = run(
        forward_one,
        [
            kept((rows * chan, wide)),
            kept((devices, SECOND, 128), BF16),
            kept((ext * 3 * chan, wide), BF16),
            kept((128, wide), BF16),
            kept((BAND, RIM)),
            kept((2 * chan + 16, 128)),
            kept((8, 128)),
        ],
        [
            pltpu.VMEM((ext * chan, wide), F32),
            pltpu.VMEM((devices * FIRST, 128), F32),
            pltpu.VMEM((n_tm * 8, 128), F32),
            pltpu.VMEM((mels + 8, RIM), F32),
            pltpu.VMEM((devices * SECOND, 128), F32),
        ],
        recv,
        spec,
        pairs,
        singles,
        twice,
        w1,
        wf,
        params,
        masks,
        all_masks,
        edge_masks,
    )
    recv = exchange(payload)
    grad, kept_half, sent_half, totals, stats_two, row_pairs = run(
        backward_scaled,
        [
            kept((rows * chan, frame_dev)),
            kept((TAPS // 2 + devices, 128)),
            kept((TAPS // 2 + devices, 128)),
            kept((8, 128)),
            kept((chan + 8, 128)),
            kept((rows // 2 * chan, frame_dev)),
        ],
        [
            pltpu.VMEM((rows // 2 * chan, frame_dev), F32),
            pltpu.VMEM((3 * chan + 16, rows * frame_dev), BF16),
            pltpu.VMEM((2, TAPS // 2 + devices, 128), F32),
        ],
        recv,
        pre_two,
        act,
        own_rows,
        params,
        masks,
    )
    received = lax.ppermute(sent_half, "tm", [(i, i ^ 1) for i in range(n_tm)])
    pre_ring, ring, rim = run(
        around,
        [kept((4 * chan, wide)), kept((4 * chan, wide)), kept((rows * chan, RIM))],
        [
            pltpu.VMEM(((rows // 2 + 2) * chan, RIM), F32),
            pltpu.VMEM((2 * chan, frame_dev), F32),
            pltpu.VMEM((devices * SECOND, 128), F32),
            pltpu.VMEM((2 * chan, half), F32),
            pltpu.VMEM((4 * 3 * chan, wide), BF16),
        ],
        recv,
        pre_two,
        act,
        w1,
        wf,
        x3,
        far_rim,
        stats_one,
        masks,
        stats_two,
    )
    (payload,) = run(
        pack_sums,
        [kept((devices * (half_share(devices, 9 * chan) + 2), 128))],
        [],
        kept_half,
        received,
        totals,
        rim,
    )
    recv = exchange_rows(payload)
    grad, own_low, payload, totals = run(
        backward,
        [
            kept(((rows + 4) * chan, wide), BF16),
            kept((rows * chan, frame_dev), BF16),
            kept((devices, LAST, 128), BF16),
            kept((8, 128)),
        ],
        [
            pltpu.VMEM(((rows + 2) * 3 * chan, frame_dev), BF16),
            pltpu.VMEM((rows * chan, frame_dev), F32),
            pltpu.VMEM((rows * chan, 2 * frame_dev), BF16),
        ],
        recv,
        pre_two,
        pre_ring,
        grad,
        ring,
        rim,
        stats_two,
        w1,
        x3,
        stats_one,
        params,
        masks,
        wb,
    )
    recv = exchange(payload)
    pooled, gain_two_grad, bias_two_grad = run(
        pool,
        [shape((1, chan, rows // 2, half), BF16), shape((1, chan)), shape((1, chan))],
        [
            pltpu.VMEM((rows // 2 * chan, 128), F32),
        ],
        totals,
        row_pairs,
    )
    first, ws, normed_taps = run(
        transposed,
        [
            kept((rows * 3, wide)),
            kept((rows * 3, (rows + 2) * chan), BF16),
            kept((32, chan)),
        ],
        [
            pltpu.VMEM(((rows + 2) * chan, wide), BF16),
            pltpu.VMEM((8 * 3 * chan, frame_dev), BF16),
            pltpu.VMEM(((rows + 4) * 3 * chan, RIM), BF16),
            pltpu.SemaphoreType.DMA,
        ],
        grad,
        own_low,
        w1,
        wb,
        x3,
        stats_one,
        features,
        k1t,
        params,
        masks,
        ws,
        hbm=1,
    )
    spec_grad, kernel_one_grad, kernel_two_grad, gain_one_grad, bias_one_grad = run(
        finish,
        [
            shape((1, rows, frame_dev)),
            shape((3, 3, chan)),
            shape((9, chan, chan)),
            shape((1, chan)),
            shape((1, chan)),
        ],
        [
            pltpu.VMEM((1, rows, frame_dev), F32),
            pltpu.VMEM((3, 3, chan), F32),
            pltpu.VMEM((9, chan, chan), F32),
            pltpu.VMEM((1, chan), F32),
            pltpu.VMEM((1, chan), F32),
            pltpu.VMEM((devices * LAST, 128), F32),
            pltpu.SemaphoreType.DMA((5,)),
        ],
        recv,
        features,
        stats_one,
        k1t,
        first,
        ws,
        w1,
        x3,
        normed_taps,
        params,
        masks,
        apart=range(5),
    )
    kernel_two_grad = jnp.transpose(kernel_two_grad.reshape(3, 3, chan, chan), (2, 3, 0, 1))
    return (
        pooled,
        spec_grad,
        jnp.transpose(kernel_one_grad, (2, 0, 1)),
        gain_one_grad[0],
        bias_one_grad[0],
        kernel_two_grad,
        gain_two_grad[0],
        bias_two_grad[0],
    )


def solution(mesh):
    return jax.shard_map(
        shards,
        mesh=mesh,
        in_specs=(
            P(None, "mel", "tm"),
            P(),
            P(),
            P(),
            P(),
            P(),
            P(),
            P(),
            P(None, None, "mel", "tm"),
        ),
        out_specs=(P(None, None, "mel", "tm"), P(None, "mel", "tm"), P(), P(), P(), P(), P(), P()),
        check_vma=False,
    )
```

```python
import math

import jax
import jax.numpy as jnp
from jax import lax
from jax.experimental import pallas as pl
from jax.experimental.pallas import tpu as pltpu
from jax.sharding import PartitionSpec as P

F32 = jnp.float32
BF16 = jnp.bfloat16
AXES = ("mel", "tm")
EXACT = lax.Precision.HIGHEST
RIM = 128
BAND = 24
MEL_ROWS = 16
FIRST = 16
SUMS, EDGES, COLUMNS = 8, 11, 15
SIDE, FAR = 96, 112
FAR_HOLDERS = 32
LAST = 24
TAPS = 576
SECOND = 8


def iota(shape, dim):
    return lax.broadcasted_iota(jnp.int32, shape, dim)


def dot(a, b, over=((1,), (0,)), precision=None):
    return lax.dot_general(a, b, (over, ((), ())), precision=precision, preferred_element_type=F32)


def to_column(lanes, count, start=0):
    shape = (count, lanes.shape[1])
    return jnp.sum(jnp.where(iota(shape, 1) == iota(shape, 0) + start, lanes, 0.0), axis=1, keepdims=True)


def to_lanes(column, start=0, width=128):
    shape = (column.shape[0], width)
    return jnp.sum(jnp.where(iota(shape, 1) == iota(shape, 0) + start, column, 0.0), axis=0, keepdims=True)


def halves(v):
    total = v[:, :128]
    for n in range(128, v.shape[1], 128):
        total = total + v[:, n : n + 128]
    return total


def frame_masks(bounds, frames):
    last = bounds.shape[1] - 1
    end = bounds[:, last:]

    def living(f):
        return (f >= 0) & (f < end)

    def paired(f):
        both = living(f) & living(f + 1)
        for k in range(1, last):
            both = both & (f + 1 != bounds[:, k : k + 1])
        return both

    return tuple(m.astype(F32) for m in (living(frames), paired(frames - 1), paired(frames)))


def row_valid(row, rows):
    mel = lax.axis_index("mel") * rows + row
    return ((mel >= 0) & (mel < lax.axis_size("mel") * rows)).astype(F32)


def start_all(*pairs, sems):
    copies = [pltpu.make_async_copy(src, dst, sems.at[n]) for n, (src, dst) in enumerate(pairs)]
    for copy in copies:
        copy.start()
    return copies


def wait_all(copies):
    for copy in copies:
        copy.wait()


def shifted_frames(value, behind, ahead):
    wide = value.shape[1]
    return pltpu.roll(value, 1, 1) * behind, pltpu.roll(value, wide - 1, 1) * ahead


def three_parts(v):
    high = lax.reduce_precision(v, 8, 7)
    mid = lax.reduce_precision(v - high, 8, 7)
    return high, mid, v - high - mid


def share_of(devices, chan):
    return -(-chan // devices)


def pack(spec_hbm, grad_hbm, bounds_hbm, out, own, spec, masks, bounds, edges, rows_out, sems):
    copies = start_all((bounds_hbm, bounds), (spec_hbm, spec), (grad_hbm, own), sems=sems)
    copies[0].wait()
    wide = masks.shape[1]
    frame_dev = wide - RIM
    devices = out.shape[0]
    rows = MEL_ROWS
    lane = iota((1, wide), 1)
    frames = lax.axis_index("tm") * frame_dev + jnp.where(lane < frame_dev + RIM // 2, lane, lane - wide)
    last = bounds.shape[1] - 1
    pixels = bounds[:, last:].astype(F32) * (lax.axis_size("mel") * rows)
    found = frame_masks(bounds[...], frames)
    masks[...] = jnp.concatenate(
        list(found) + [jnp.full((1, wide), 1.0) * pixels, jnp.zeros((4, wide), F32)], axis=0
    )
    usable, behind, ahead = (m[:, :frame_dev] for m in found)
    copies[1].wait()
    copies[2].wait()
    x = spec[0].astype(F32) * usable
    lane = iota((1, frame_dev), 1)
    row = iota((rows, 1), 0)
    inner = jnp.where((lane > 0) & (lane < frame_dev - 1), usable, 0.0)
    number = (rows - 2) * jnp.sum(inner, axis=1, keepdims=True)
    inner = inner * ((row > 0) & (row < rows - 1)).astype(F32)
    centre = jnp.sum(jnp.sum(x, axis=0, keepdims=True), axis=1, keepdims=True)
    centre = centre / (rows * jnp.maximum(jnp.sum(usable, axis=1, keepdims=True), 1.0))
    centre = lax.reduce_precision(centre, 8, 7)
    shifted = [pltpu.roll(x, 1, 1) * behind, x, pltpu.roll(x, frame_dev - 1, 1) * ahead]
    taps = [pltpu.roll(v, (1 - i) % rows, 0) if i != 1 else v for i in range(3) for v in shifted]
    features = feature_rows(centre, (taps, inner))
    lane = iota((1, 128), 1)
    features = jnp.where(lane == 90, centre, jnp.where(lane == 91, number, features))
    pick = iota((8, frame_dev), 0)
    column = jnp.where(pick < 4, pick, frame_dev - 8 + pick)
    strip = dot((iota((8, frame_dev), 1) == column).astype(BF16), x.astype(BF16), ((1,), (1,)))
    lane = iota((8, 128), 1)
    repeat = (iota((rows, 128), 1) % rows == iota((rows, 128), 0)).astype(BF16)
    strip = jnp.where(lane // rows == iota((8, 128), 0), dot(strip.astype(BF16), repeat), 0.0)
    strip = jnp.sum(strip, axis=0, keepdims=True)

    def put(n, value):
        rows_out[pl.ds(n, devices, stride=FIRST), :] = jnp.broadcast_to(value, (devices, 128))

    near = jnp.concatenate([x[0:2], x[rows - 2 :]], axis=0)
    near = jnp.concatenate([near[:, :128], near[:, 128:]], axis=0)
    for d in range(devices):
        rows_out[FIRST * d : FIRST * d + 8, :] = near
    put(COLUMNS, strip)
    _, chan, many, half = own.shape
    share = share_of(devices, chan)
    holders = chan // share
    g = own[0].astype(F32)
    edges[0:chan] = g[:, 0, :]
    edges[chan:] = g[:, many - 1, :]

    def spread_out(v, held):
        if held < devices:
            v = jnp.concatenate([v, jnp.zeros((devices - held, 128), F32)], axis=0)
        return v

    for n in range(share):
        put(EDGES + n, spread_out(edges[n * holders : (n + 1) * holders, :], holders))
        put(EDGES + share + n, spread_out(edges[chan + n * holders : chan + (n + 1) * holders, :], holders))
    for n in range(2 * share, COLUMNS - EDGES):
        put(EDGES + n, jnp.zeros((1, 128), F32))
    end = iota((8, half), 0)
    at = iota((8, half), 1)
    ends = ((end == 0) & (at == 0)) | ((end == 1) & (at == half - 1))
    columns = dot(ends.astype(BF16), g.reshape(chan * many, half).astype(BF16), ((1,), (1,)))
    group = 128 // many
    source = iota((128, 128), 0)
    lane = iota((group, 128), 1)
    mine = lane // many == iota((group, 128), 0)
    lane8, own8 = iota((8, 128), 1), iota((8, 128), 0)
    parts = three_parts(features)
    for n in range(2):
        side = jnp.zeros((holders, 128), F32)
        for m in range(share):
            move = (iota((128, 128), 1) == SIDE + many * m + source % many).astype(BF16)
            first = m * holders * many // 128
            block = [columns[n : n + 1, 128 * q : 128 * (q + 1)] for q in range(first, first + holders * many // 128)]
            block = jnp.concatenate([jnp.where(mine, v, 0.0) for v in block], axis=0)
            side = side + dot(block.astype(BF16), move)
        far = x[2:4] if n == 0 else x[rows - 4 : rows - 2]
        pieces = [far[r : r + 1, 128 * h : 128 * (h + 1)] for r in range(2) for h in range(2)]
        pieces = jnp.concatenate([jnp.where(lane8 // 16 == own8, v, 0.0) for v in pieces], axis=0)
        far = dot(pieces.astype(BF16), (iota((128, 128), 1) == FAR + source % 16).astype(BF16))
        put(SUMS + n, spread_out(side, holders) + spread_out(far, FAR_HOLDERS) + parts[n])
    put(SUMS + 2, parts[2])
    out[...] = rows_out[...].reshape(out.shape).astype(BF16)


def weights(own, bounds_hbm, k2_hbm, k1_hbm, gain_one_hbm, bias_one_hbm, gain_two_hbm, bias_two_hbm,
            wf, wb, w1, ws_hbm, pairs, singles, k1t, params, all_masks, edge_masks, twice, own_rows,
            k2, k1, vectors, bounds, ws, temp, sems):
    loads = start_all(
        (bounds_hbm, bounds),
        (k2_hbm, k2),
        (k1_hbm, k1),
        (gain_one_hbm, vectors.at[0]),
        (bias_one_hbm, vectors.at[1]),
        (gain_two_hbm, vectors.at[2]),
        (bias_two_hbm, vectors.at[3]),
        sems=sems,
    )
    _, many, count, half = own.shape
    temp[...] = own[0].astype(F32).reshape(many * count, half)
    for r in range(count):
        own_rows[r * many : (r + 1) * many] = temp[pl.ds(r, many, stride=count), :].astype(BF16)
    wait_all(loads)
    chan = k2.shape[1]
    span = wf.shape[1]
    taps = [k2[t].astype(F32) for t in range(9)]
    rest = jnp.zeros((chan, span - 9 * chan), F32)
    forward = jnp.concatenate(taps + [rest], axis=1)
    backward = jnp.concatenate([taps[8 - t].T for t in range(9)] + [rest], axis=1)
    for r in range(wb.shape[0] // chan):
        at = slice(r * chan, (r + 1) * chan)
        wb[at] = (pltpu.roll(backward, 3 * chan * r, 1) if r else backward).astype(BF16)
    full = jnp.concatenate([k1[n].astype(F32) for n in range(3)] + [jnp.zeros((7, chan), F32)], axis=0)
    low = [
        jnp.concatenate([full[3 * (2 - a) + 2 - b : 3 * (2 - a) + 3 - b] for a in range(3)], axis=1)
        for b in range(3)
    ]
    rest = jnp.zeros((1, ws.shape[1] - 3 * chan), F32)
    for b in range(3):
        base = jnp.concatenate([low[b], rest], axis=1)
        many = ws.shape[0] // 3
        rolled = [pltpu.roll(base, chan * m, 1) if m else base for m in range(many)]
        ws[many * b : many * (b + 1)] = jnp.concatenate(rolled, axis=0).astype(BF16)
    store_ws = pltpu.make_async_copy(ws, ws_hbm, sems.at[7])
    store_ws.start()
    count, frame_dev = all_masks.shape[0] // 3, all_masks.shape[1]
    frames = iota((count, frame_dev), 0) * frame_dev + iota((count, frame_dev), 1)
    for n, mask in enumerate(frame_masks(bounds[...], frames)):
        all_masks[n * count : (n + 1) * count] = mask
    q = iota(edge_masks.shape, 0)
    lane = iota(edge_masks.shape, 1)
    k = q % 8
    frames = (q // 8) * frame_dev + jnp.where(k < 4, k, k + frame_dev - 8)
    living, behind, ahead = frame_masks(bounds[...], frames)
    living = jnp.where((k == 0) | (k == 7), living, 0.0)
    edge_masks[...] = jnp.where(lane == 0, living, jnp.where(lane == 1, behind, jnp.where(lane == 2, ahead, 0.0)))
    params[...] = jnp.concatenate(
        [vectors[n] for n in range(4)] + [jnp.zeros((4, chan), F32)], axis=0
    )
    tap = iota((16, 128), 0)
    lane = iota((16, 128), 1)
    i = (tap * 11) >> 5
    ninth = (lane * 57) >> 9
    to_band = (lane == BAND * (tap - 3 * i) + i) & (tap < 9)
    to_left = (ninth == tap) & (tap < 9)
    to_right = (lane - 9 * ninth == tap) & (lane < 81)
    to_single = (lane == 81 + tap) & (tap < 9)
    source = iota((128, 128), 0) - 81
    lane = iota((128, 128), 1)
    ninth = (lane * 57) >> 9
    inside = (source >= 0) & (source < 9) & (lane < 81)
    twice[...] = jnp.where(inside, (source == ninth).astype(F32) + (source == lane - 9 * ninth).astype(F32), 0.0)
    for r in range(wf.shape[0] // chan):
        at = slice(r * chan, (r + 1) * chan)
        wf[at] = (pltpu.roll(forward, 3 * chan * r, 1) if r else forward).astype(BF16)
    k1t[...] = full
    k = full.astype(BF16)
    lanes = [dot(k, select.astype(BF16), ((0,), (0,))) for select in (to_band, to_left, to_right, to_single)]
    pairs[...] = lanes[1] * lanes[2]
    singles[...] = lanes[3]
    for m in range(w1.shape[0] // chan):
        w1[m * chan : (m + 1) * chan] = (pltpu.roll(lanes[0], m, 1) if m else lanes[0]).astype(BF16)
    store_ws.wait()


def feature_rows(centre, *parts):
    def folded(v):
        return jnp.sum(halves(v), axis=0, keepdims=True)

    rows = [jnp.zeros((1, 128), F32)] * 96
    for taps, weight in parts:
        z = [tap - centre for tap in taps]
        for s in range(9):
            left = z[s] * weight
            rows[81 + s] = rows[81 + s] + folded(left)
            for t in range(s, 9):
                rows[9 * s + t] = rows[9 * t + s] = rows[9 * s + t] + folded(left * z[t])
    return to_lanes(jnp.sum(jnp.concatenate(rows, axis=0), axis=1, keepdims=True))


def summed_blocks(ref, devices, by=1):
    block = ref.shape[0] // devices
    period = max(8 // math.gcd(block, 8), by)
    step = period * block
    total = ref[0:step, :]
    for at in range(step, ref.shape[0], step):
        total = total + ref[at : at + step, :]
    results = []
    for first in range(by):
        result = total[first * block : (first + 1) * block]
        for n in range(first + by, period, by):
            result = result + total[n * block : (n + 1) * block]
        results.append(result)
    return results if by > 1 else results[0]


def moved_rows(v, step):
    if step == 0:
        return v
    count = v.shape[0]
    if abs(step) >= count:
        return jnp.zeros_like(v)
    zero = jnp.zeros((abs(step), v.shape[1]), v.dtype)
    if step > 0:
        return jnp.concatenate([zero, v[: count - step]], axis=0)
    return jnp.concatenate([v[-step:], zero], axis=0)


def silu_halves(h):
    t = jnp.tanh(h)
    one = 1.0 + t
    return h * one, one * (1.0 + h * (1.0 - t))


def act_row(act, r, low, low_masks):
    low = low * low_masks[0]
    chan = low.shape[0]
    for n, v in enumerate((low,) + shifted_frames(low, *low_masks[1:])):
        at = (3 * r + (1, 0, 2)[n]) * chan
        act[at : at + chan, :] = v


def forward_one(recv, spec, pairs, singles, twice, w1, wf, params, masks, all_masks, edge_masks,
                pre_two, payload, act, x3, far_rim, stats, features_out, pre_one, got, strips, halo, rows_out):
    devices = recv.shape[0]
    n_mel, count = lax.axis_size("mel"), lax.axis_size("tm")
    rows = MEL_ROWS
    mels = n_mel * rows
    wide = masks.shape[1]
    frame_dev = wide - RIM
    chan = params.shape[1]
    me_m, me_t = lax.axis_index("mel"), lax.axis_index("tm")
    usable, behind, ahead = (masks[n : n + 1] for n in range(3))
    total = masks[3:4, 0:1]
    got[...] = recv[...].astype(F32).reshape(devices * FIRST, 128)

    def every(n):
        return got[pl.ds(n, devices, stride=FIRST), :]

    lane = iota((count, 128), 1)
    bands = [got[pl.ds(FIRST * k * count + COLUMNS, count, stride=FIRST), :] for k in range(n_mel)]
    for c in range(8):
        column = jnp.zeros((count, 128), F32)
        for k, band in enumerate(bands):
            part = jnp.where(lane // rows == c, band, 0.0)
            column = column + (pltpu.roll(part, rows * (k - c) % 128, 1) if k != c else part)
        strips[pl.ds(c, count, stride=8), :] = column
    at = pl.multiple_of(FIRST * (jnp.maximum(me_m - 1, 0) * count + me_t), 8)
    above = got[pl.ds(at, 8), :] * (me_m > 0).astype(F32)
    at = pl.multiple_of(FIRST * (jnp.minimum(me_m + 1, n_mel - 1) * count + me_t), 8)
    below = got[pl.ds(at, 8), :] * (me_m < n_mel - 1).astype(F32)
    above = jnp.concatenate([above[2:4], above[6:8]], axis=1)
    below = jnp.concatenate([below[0:2], below[4:6]], axis=1)
    own = spec[0].astype(F32) * usable[:, :frame_dev]
    at = pl.multiple_of(8 * jnp.minimum(me_t + 1, count - 1), 8)
    after = strips[pl.ds(at, 8), :][:, :mels] * (me_t + 1 < count).astype(F32)
    at = pl.multiple_of(8 * jnp.maximum(me_t - 1, 0), 8)
    before = strips[pl.ds(at, 8), :][:, :mels] * (me_t > 0).astype(F32)
    sides = jnp.concatenate([after[0:4], before[4:8], jnp.zeros((8, mels), F32)], axis=0).astype(BF16)
    side = iota((16, RIM), 0)
    place = iota((16, RIM), 1) == jnp.where(side < 4, side, jnp.where(side < 8, side + RIM - 8, -1))
    halo[0:8] = jnp.zeros((8, RIM), F32)
    halo[mels : mels + 8] = jnp.zeros((8, RIM), F32)
    halo[4 : mels + 4] = dot(sides, place.astype(BF16), ((0,), (0,)))
    rim = halo[pl.ds(pl.multiple_of(me_m * rows, 8), BAND), :]
    far_rim[...] = rim
    row = iota((BAND, RIM), 0)
    rim = jnp.where((row >= 2) & (row < BAND - 2), rim, 0.0)
    blank = jnp.zeros((2, frame_dev), F32)
    near = jnp.concatenate([jnp.concatenate([blank, above, own, below, blank], axis=0), rim], axis=1)
    x3[...] = jnp.concatenate(
        [
            pltpu.roll(near, 1, 1) * behind,
            near,
            pltpu.roll(near, wide - 1, 1) * ahead,
            jnp.broadcast_to(usable, (BAND, wide)),
            jnp.zeros((128 - 4 * BAND, wide), F32),
        ],
        axis=0,
    ).astype(BF16)
    pre_one[2 * chan : (rows + 4) * chan] = dot(w1[2 * chan : (rows + 4) * chan, :], x3[...])
    lane = iota((1, 128), 1)
    parts = jnp.where(lane < 92, every(SUMS) + every(SUMS + 1) + every(SUMS + 2), 0.0)
    centres, numbers = parts[:, 90:91], parts[:, 91:92]
    centre = jnp.sum(centres * numbers, axis=0, keepdims=True)
    centre = centre / jnp.maximum(jnp.sum(numbers, axis=0, keepdims=True), 1.0)
    delta = centres - centre
    features = jnp.sum(parts + delta * numbers * jnp.where(lane < 81, delta, 1.0), axis=0, keepdims=True)
    moved = jnp.sum(delta * parts, axis=0, keepdims=True)
    def edge_row(k, n):
        first = FIRST * k * count + n
        return jnp.concatenate(
            [got[pl.ds(first, count, stride=FIRST), :], got[pl.ds(first + 4, count, stride=FIRST), :]], axis=1
        )

    edge_rows = [[edge_row(k, n) for n in range(4)] for k in range(n_mel)]
    zero = jnp.zeros((count, frame_dev), F32)
    rows_of = [[], [], []]
    for k, (top, second, fore, bottom) in enumerate(edge_rows):
        for n, v in enumerate((edge_rows[k - 1][3] if k else zero, top, second)):
            rows_of[n].append(v)
        for n, v in enumerate((fore, bottom, edge_rows[k + 1][0] if k + 1 < n_mel else zero)):
            rows_of[n].append(v)
    f_usable, f_behind, f_ahead = (all_masks[n * count : (n + 1) * count, :] for n in range(3))
    lane = iota((count, frame_dev), 1)

    def frame_before(v):
        v = pltpu.roll(v, 1, 1)
        return jnp.where(lane == 0, pltpu.roll(v, 1, 0), v) * f_behind

    def frame_after(v):
        v = pltpu.roll(v, frame_dev - 1, 1)
        return jnp.where(lane == frame_dev - 1, pltpu.roll(v, count - 1, 0), v) * f_ahead

    taps = []
    for group in rows_of:
        for move in (frame_before, lambda v: v, frame_after):
            taps.append(jnp.concatenate([move(v) for v in group], axis=1))
    f_usable = jnp.concatenate([f_usable] * (2 * n_mel), axis=1)
    borders = (taps, f_usable)
    edge = strips[...]
    q_usable, q_behind, q_ahead = (edge_masks[:, n : n + 1] for n in range(3))
    lane = iota((count * 8, 128), 1)
    inside = (lane < mels) & (lane % rows != 0) & (lane % rows != rows - 1)
    shifted = [
        pltpu.roll(edge, 1, 0) * q_behind,
        edge,
        pltpu.roll(edge, count * 8 - 1, 0) * q_ahead,
    ]
    taps = [pltpu.roll(v, (1 - i) % 128, 1) if i != 1 else v for i in range(3) for v in shifted]
    features = features + feature_rows(centre, borders, (taps, jnp.where(inside, q_usable, 0.0)))
    features = jnp.where(iota((1, 128), 1) < 90, features, 0.0)
    near_mean = jnp.sum(singles[...] * features, axis=1, keepdims=True) / total
    around = jnp.sum(singles[...], axis=1, keepdims=True)
    square = jnp.sum(pairs[...] * features, axis=1, keepdims=True)
    square = (square + 2.0 * around * jnp.sum(singles[...] * moved, axis=1, keepdims=True)) / total
    inv = lax.rsqrt(square - near_mean * near_mean + 1e-05)
    mean = near_mean + centre * around
    lane = iota((chan, 128), 1)
    stats[0:chan] = jnp.where(lane == 0, mean, jnp.where(lane == 1, inv, 0.0))
    stats[chan : chan + 8] = jnp.broadcast_to(to_lanes(near_mean), (8, 128))
    stats[chan + 8 : chan + 16] = jnp.broadcast_to(to_lanes(inv), (8, 128))
    scale = 0.5 * to_column(params[0:1], chan) * inv
    shift = 0.5 * to_column(params[1:2], chan) - mean * scale
    stats[chan + 16 :] = jnp.where(lane == 0, scale, jnp.where(lane == 1, shift, 0.0))
    scale = jnp.broadcast_to(scale, (chan, wide))
    shift = jnp.broadcast_to(shift, (chan, wide))
    block, taps = wf.shape
    first = jnp.zeros((chan, 128), F32)
    second = jnp.zeros((chan, 128), F32)
    own_mask = usable[:, :frame_dev]
    low_masks = [m.astype(BF16) for m in (usable, behind, ahead)]
    for r in range(2, rows + 4):
        value, _ = silu_halves(pre_one[r * chan : (r + 1) * chan, :] * scale + shift)
        if not 0 <= r - 3 < rows:
            value = value * row_valid(r - 3, rows)
        act_row(act, r, value.astype(BF16), low_masks)
        if r < 5 or r % 2 == 0:
            continue
        g = (r - 3) // 2
        result = dot(wf[...], act[g * 3 * block : g * 3 * block + taps, :frame_dev])
        at = (g - 1) * block
        pre_two[at : at + block, :frame_dev] = result
        if g % 2 == 0:
            beside = [act[n * 3 * block : n * 3 * block + taps, frame_dev:] for n in (g - 1, g)]
            beside = dot(wf[...], jnp.concatenate(beside, axis=1))
            for n in range(2):
                pre_two[at + (n - 1) * block : at + n * block, frame_dev:] = beside[:, n * RIM : (n + 1) * RIM]
        for q in range(2):
            p = result[q * chan : (q + 1) * chan]
            masked = p * own_mask
            first = first + halves(masked)
            second = second + halves(masked * p)
    moved = dot(jnp.broadcast_to(moved, (8, 128)), twice[...], precision=EXACT)[0:1]
    features_out[...] = jnp.concatenate(
        [features + moved, jnp.broadcast_to(centre, (1, 128)), jnp.zeros((6, 128), F32)], axis=0
    )
    share = share_of(devices, chan)

    def put(n, value):
        rows_out[pl.ds(n, devices, stride=SECOND), :] = jnp.broadcast_to(value, (devices, 128))

    for n in range(share):
        put(3 + n, moved_rows(every(EDGES + share + n), count))
        put(3 + share + n, moved_rows(every(EDGES + n), -count))
    for n in [0, 1, 2] + list(range(3 + 2 * share, SECOND - 1)):
        put(n, jnp.zeros((1, 128), F32))
    lane = iota((devices, 128), 1)
    tm = iota((devices, 128), 0) % count
    at_side = (lane >= SIDE) & (lane < FAR)
    lefts = jnp.where(at_side, every(SUMS), 0.0)
    rights = jnp.where(at_side, every(SUMS + 1), 0.0)
    beside = jnp.zeros((devices, 128), F32)
    for n, step in enumerate((0, count, -count)):
        one = jnp.where(tm > 0, moved_rows(rights, step + 1), 0.0)
        two = jnp.where(tm < count - 1, moved_rows(lefts, step - 1), 0.0)
        beside = beside + pltpu.roll(one, (32 * n - SIDE) % 128, 1) + pltpu.roll(two, (32 * n + 16 - SIDE) % 128, 1)
    outer = jnp.where(lane >= FAR, moved_rows(every(SUMS + 1), count), 0.0)
    beside = beside + pltpu.roll(outer, 128 - 16, 1)
    beside = beside + jnp.where(lane >= FAR, moved_rows(every(SUMS), -count), 0.0)
    put(SECOND - 1, beside)
    first = jnp.sum(first, axis=1, keepdims=True)
    second = jnp.sum(second, axis=1, keepdims=True)
    parts = list(three_parts(to_lanes(first) + to_lanes(second, chan)))
    parts = jnp.concatenate(parts + [jnp.zeros((SECOND - 3, 128), F32)], axis=0)
    for d in range(devices):
        payload[d] = (rows_out[SECOND * d : SECOND * (d + 1), :] + parts).astype(BF16)


def spreading(half):
    lane = iota((half, 2 * half), 1)
    return jnp.where(lane >> 1 == iota((half, 2 * half), 0), 0.25, 0.0).astype(BF16)


def half_share(devices, taps):
    return -(-taps // 2 // devices)


def backward_scaled(recv, pre_two, act, own_rows, params, masks,
                    grad, kept_half, sent_half, totals, stats, pairs, up, right, halved):
    devices = recv.shape[0]
    chan = params.shape[1]
    half = own_rows.shape[1]
    frame_dev = 2 * half
    rows = MEL_ROWS
    up[...] = dot(own_rows[...], spreading(half))
    usable = masks[0:1, :frame_dev]
    total = masks[3:4, 0:1]
    sums = [recv[d].astype(F32) for d in range(devices)]
    while len(sums) > 1:
        sums = [a + b for a, b in zip(sums[0::2], sums[1::2])]
    sums = jnp.sum(sums[0][0:3], axis=0, keepdims=True)
    mean = to_column(sums, chan) / total
    inv = lax.rsqrt(to_column(sums, chan, chan) / total - mean * mean + 1e-05)
    scale = 0.5 * to_column(params[2:3], chan) * inv
    shift = 0.5 * to_column(params[3:4], chan) - mean * scale
    lane = iota((chan, 128), 1)
    columns = jnp.zeros((chan, 128), F32)
    for n, column in enumerate((mean, inv, scale, shift)):
        columns = jnp.where(lane == n, column, columns)
    stats[0:chan] = columns
    stats[chan : chan + 8] = jnp.broadcast_to(to_lanes(inv), (8, 128))
    mean, inv, scale, shift = (jnp.broadcast_to(v, (chan, frame_dev)) for v in (mean, inv, scale, shift))
    first = jnp.zeros((chan, 128), F32)
    second = jnp.zeros((chan, 128), F32)
    mask = 0.5 * usable
    right[3 * chan :] = jnp.ones((16, rows * frame_dev), BF16)
    table = jnp.zeros((9 * chan, 3 * chan + 16), F32)
    for m in range(rows):
        at = slice(m * chan, (m + 1) * chan)
        pre = pre_two[at, :frame_dev]
        value, slope = silu_halves(pre * scale + shift)
        value = value * usable
        both = value if m % 2 == 0 else both + value
        if m % 2:
            pairs[m // 2 * chan : (m // 2 + 1) * chan, :] = both
        g = up[m // 2 * chan : (m // 2 + 1) * chan, :] * slope * mask
        grad[at, :] = g
        normed = (pre - mean) * inv
        first = first + halves(g * normed)
        second = second + halves(g)
        lanes = slice(m * frame_dev, (m + 1) * frame_dev)
        right[0:chan, lanes] = g.astype(BF16)
        right[chan : 2 * chan, lanes] = normed.astype(BF16)
        right[2 * chan : 3 * chan, lanes] = (g - right[0:chan, lanes].astype(F32)).astype(BF16)
        if m in (5, 11, rows - 1):
            start = m - m % 6
            left = [act[(n + 2) * 3 * chan : (n + 5) * 3 * chan, :frame_dev] for n in range(start, m + 1)]
            lanes = slice(start * frame_dev, (m + 1) * frame_dev)
            table = table + dot(jnp.concatenate(left, axis=1), right[:, lanes], ((1,), (1,)))
    first = jnp.sum(first, axis=1, keepdims=True)
    second = jnp.sum(second, axis=1, keepdims=True)
    totals[...] = jnp.broadcast_to(to_lanes(first) + to_lanes(second, chan), (8, 128))
    rest = jnp.concatenate([table[:, 2 * chan :], jnp.zeros((9 * chan, chan - 16), F32)], axis=1)
    both = table[:, : 2 * chan] + jnp.where(iota(rest.shape, 1) < chan, rest, 0.0)
    single = rest[:, chan : chan + 1]
    taps = 9 * chan // 2
    lane = iota((devices, 128), 1)
    for h in range(2):
        halved[h, 0:taps] = both[h * taps : (h + 1) * taps]
        constants = jnp.zeros((devices, 128), F32)
        for k in range(half_share(devices, 9 * chan)):
            at = h * taps + k * devices
            ones = single[at : min(at + devices, (h + 1) * taps)]
            if ones.shape[0] < devices:
                ones = jnp.concatenate([ones, jnp.zeros((devices - ones.shape[0], 1), F32)], axis=0)
            constants = jnp.where(lane == k, ones, constants)
        halved[h, taps:] = constants
    core = lax.axis_index("tm") % 2
    kept_half[...] = halved[core]
    sent_half[...] = halved[1 - core]


def around(recv, pre_two, act, w1, wf, x3, far_rim, stats_one, masks, stats, pre_ring, ring, rim,
           sides, up, got, beyond, more):
    devices = recv.shape[0]
    got[...] = recv[:, 0:SECOND, :].astype(F32).reshape(devices * SECOND, 128)
    rows = MEL_ROWS
    many = rows // 2
    wide = pre_two.shape[1]
    frame_dev = wide - RIM
    chan = pre_two.shape[0] // rows
    usable = masks[0:1]
    low_masks = [masks[n : n + 1].astype(BF16) for n in range(3)]
    pieces = got[pl.ds(SECOND - 1, devices, stride=SECOND), :][:FAR_HOLDERS].astype(BF16)
    source = iota((128, 128), 0)
    lane = iota((FAR_HOLDERS, 128), 1)
    mine = lane // 16 == iota((FAR_HOLDERS, 128), 0) % 8
    outer = []
    for first in (SIDE, FAR):
        place = (source - first == iota((128, 128), 1) % 16).astype(BF16)
        v = jnp.where(mine, dot(pieces, place), 0.0)
        v = [jnp.sum(v[8 * n : 8 * n + 8], axis=0, keepdims=True) for n in range(4)]
        outer += [jnp.concatenate(v[2 * r : 2 * r + 2], axis=1) for r in range(2)]
    blank = jnp.zeros((BAND - 4, frame_dev), F32)
    far = jnp.concatenate(outer[:2] + [blank] + outer[2:], axis=0)
    row = iota((BAND, RIM), 0)
    far = jnp.concatenate([far, jnp.where((row < 2) | (row >= BAND - 2), far_rim[...], 0.0)], axis=1)
    far = jnp.concatenate(
        [
            pltpu.roll(far, 1, 1) * masks[1:2],
            far,
            pltpu.roll(far, wide - 1, 1) * masks[2:3],
            jnp.zeros((128 - 3 * BAND, wide), F32),
        ],
        axis=0,
    )
    x_all = (x3[...].astype(F32) + far).astype(BF16)
    scale = jnp.broadcast_to(stats_one[chan + 16 :, 0:1], (chan, wide))
    shift = jnp.broadcast_to(stats_one[chan + 16 :, 1:2], (chan, wide))
    for h, start in enumerate((0, rows + 4)):
        pre_one = dot(w1[start * chan : (start + 2) * chan, :], x_all)
        for n in range(2):
            value, _ = silu_halves(pre_one[n * chan : (n + 1) * chan] * scale + shift)
            value = value * row_valid(start + n - 3, rows)
            act_row(more, 2 * h + n, value.astype(BF16), low_masks)
    line = 3 * chan
    above = jnp.concatenate([more[0 : 2 * line, :], act[2 * line : 4 * line, :]], axis=0)
    below = jnp.concatenate([act[(rows + 2) * line : (rows + 4) * line, :], more[2 * line :, :]], axis=0)
    pre_ring[0 : 2 * chan] = dot(wf[...], above)
    pre_ring[2 * chan :] = dot(wf[...], below)
    share = share_of(devices, chan)
    holders = chan // share

    def every(n):
        return got[pl.ds(n, devices, stride=SECOND), :]

    beside = 0.25 * every(SECOND - 1)[:holders]
    lane = iota((holders, RIM), 1)
    for n in range(share):
        first = n * holders
        beyond[first : first + holders, :] = every(3 + n)[:holders]
        beyond[chan + first : chan + first + holders, :] = every(3 + share + n)[:holders]
        for r in range(many + 2):
            at = many * n + (r if r < many else 32 + many - 1 if r == many else 64)
            left, right_of = beside[:, at : at + 1], beside[:, at + 16 : at + 17]
            side = jnp.where(lane >= RIM - 2, left, jnp.where(lane < 2, right_of, 0.0))
            sides[r * chan + first : r * chan + first + holders, :] = side
    up[...] = dot(beyond[...].astype(BF16), spreading(frame_dev // 2))
    scale = jnp.broadcast_to(stats[0:chan, 2:3], (chan, wide))
    shift = jnp.broadcast_to(stats[0:chan, 3:4], (chan, wide))
    for n, m in enumerate((-2, -1, rows, rows + 1)):
        below = n // 2
        upstream = jnp.concatenate(
            [
                up[below * chan : (below + 1) * chan, :],
                sides[(many + below) * chan : (many + below + 1) * chan, :],
            ],
            axis=1,
        )
        _, slope = silu_halves(pre_ring[n * chan : (n + 1) * chan, :] * scale + shift)
        ring[n * chan : (n + 1) * chan, :] = upstream * slope * (usable * (0.5 * row_valid(m, rows)))
    for m in range(rows):
        at = slice(m * chan, (m + 1) * chan)
        _, slope = silu_halves(pre_two[at, frame_dev:] * scale[:, frame_dev:] + shift[:, frame_dev:])
        upstream = sides[m // 2 * chan : (m // 2 + 1) * chan, :]
        rim[m * chan : (m + 1) * chan, :] = upstream * slope * (0.5 * usable[:, frame_dev:])


def pack_sums(kept_half, received, totals, after, payload):
    del after
    devices = kept_half.shape[0] - TAPS // 2
    block = payload.shape[0] // devices
    payload[pl.ds(0, devices, stride=block), :] = jnp.broadcast_to(totals[0:1], (devices, 128))
    taps = TAPS // 2
    total = kept_half[...] + received[...]
    for k in range(block - 2):
        cut = total[k * devices : min((k + 1) * devices, taps)]
        if cut.shape[0] < devices:
            cut = jnp.concatenate([cut, jnp.zeros((devices - cut.shape[0], 128), F32)], axis=0)
        payload[pl.ds(1 + k, devices, stride=block), :] = cut
    payload[pl.ds(block - 1, devices, stride=block), :] = total[taps:]


def pool(totals, pairs, out, gain_out, bias_out, temp):
    gain_out[...] = totals[0:1, : gain_out.shape[1]]
    bias_out[...] = totals[0:1, gain_out.shape[1] :]
    chan, rows, half = out.shape[1:]
    to_mean = jnp.where(iota((2 * half, half), 0) >> 1 == iota((2 * half, half), 1), 0.25, 0.0)
    pooled = dot(pairs[...], to_mean, precision=EXACT)
    for r in range(rows):
        temp[pl.ds(r, chan, stride=rows), :] = pooled[r * chan : (r + 1) * chan]
    out[0] = temp[...].reshape(chan, rows, half).astype(BF16)


def backward(recv, pre_two, pre_ring, grad, ring, rim, stats_two, w1, x3, stats, params, masks, wb,
             out, own_low, payload, totals, g3, pre_one, g1):
    chan = params.shape[1]
    rows = MEL_ROWS
    wide = pre_two.shape[1]
    frame_dev = wide - RIM
    usable = masks[0:1]
    behind, ahead = (masks[n : n + 1].astype(BF16) for n in (1, 2))
    total = masks[3:4, 0:1]
    devices = payload.shape[0]
    pre_one[...] = dot(w1[3 * chan : (rows + 3) * chan], x3[:, :frame_dev])

    even, odd = summed_blocks(recv, devices, 2)
    sums = even[0:1] + odd[0:1]
    gain_sum, bias_sum = sums[:, :chan], sums[:, chan:]
    totals[...] = jnp.broadcast_to(sums, (8, 128))
    mean, inv = stats_two[0:chan, 0:1], stats_two[0:chan, 1:2]
    factor = to_column(params[2:3], chan) * inv
    gain_part = factor * (to_column(sums, chan) / total * inv)
    bias_part = factor * (to_column(sums, chan, chan) / total) - mean * gain_part
    gain_part = jnp.broadcast_to(gain_part, (chan, wide))
    bias_part = jnp.broadcast_to(bias_part, (chan, wide))
    factor = jnp.broadcast_to(factor, (chan, wide))
    scale = jnp.broadcast_to(stats[chan + 16 :, 0:1], (chan, frame_dev))
    shift = jnp.broadcast_to(stats[chan + 16 :, 1:2], (chan, frame_dev))
    factor_one = jnp.broadcast_to(to_column(params[0:1], chan) * stats[0:chan, 1:2], (chan, frame_dev))
    own_mask = 0.5 * usable[:, :frame_dev]
    count = rows + 4
    share = even.shape[0] - 2
    mine = jnp.concatenate([even[1 : share + 1], odd[1 : share + 1]], axis=0)
    single = jnp.concatenate([to_column(v[share + 1 :], share) for v in (even, odd)], axis=0)
    factor_l = params[2:3] * stats_two[chan : chan + 1, :chan]
    mine = mine[:, :chan] - (bias_sum * single + gain_sum * mine[:, chan:]) / total
    mine = factor_l * mine
    mine = jnp.concatenate([mine[:share], mine[share:]], axis=1)
    if share < 9:
        mine = jnp.concatenate([mine, jnp.zeros((9 - share, 128), F32)], axis=0)
    table = jnp.zeros((chan, 128), F32)

    def tap_sums(m):
        taps_in = jnp.concatenate([x3[:, :frame_dev]] * 2, axis=1)
        products = dot(g1[m * chan : (m + 4) * chan, :], taps_in, ((1,), (1,)))
        moved = [pltpu.roll(products[k * chan : (k + 1) * chan], 128 - (m + k + 3), 1) for k in range(4)]
        return (moved[0] + moved[1]) + (moved[2] + moved[3])

    for q in range(count):
        at = slice(q * chan, (q + 1) * chan)
        mask = usable if 0 <= q - 2 < rows else usable * row_valid(q - 2, rows)
        if 2 <= q < rows + 2:
            own = slice((q - 2) * chan, (q - 1) * chan)
            pre, scaled = pre_two[own, :], jnp.concatenate([grad[own, :], rim[own, :]], axis=1)
        else:
            n = q if q < 2 else q - rows
            pre, scaled = pre_ring[n * chan : (n + 1) * chan, :], ring[n * chan : (n + 1) * chan, :]
        low = (factor * scaled - (bias_part + pre * gain_part) * mask).astype(BF16)
        out[at, :] = low
        if not 1 <= q < count - 1:
            continue
        base = (q - 1) * 3 * chan
        for n, v in enumerate((low,) + shifted_frames(low, behind, ahead)):
            spot = base + (1, 0, 2)[n] * chan
            g3[spot : spot + chan, :] = v[:, :frame_dev]
        start = q - 4
        if start < 0 or start % 2:
            continue
        result = dot(wb[...], g3[start * 3 * chan : (start + 4) * 3 * chan, :])
        for n in range(2):
            m = start + n
            at = slice(m * chan, (m + 1) * chan)
            _, slope = silu_halves(pre_one[at, :] * scale + shift)
            value = result[n * chan : (n + 1) * chan] * slope * own_mask
            own_low[at, :] = (value * factor_one).astype(BF16)
            g1[at, :frame_dev] = value.astype(BF16)
            g1[at, frame_dev:] = (value - g1[at, :frame_dev].astype(F32)).astype(BF16)
        if start % 4 == 2 and start > 2:
            table = table + tap_sums(start - 6)
    table = table + tap_sums(rows - 4)
    table = table.T
    places = [BAND * j + i for i in range(3) for j in range(3)] + [3 * BAND]
    rows10 = jnp.concatenate([table[n : n + 1] for n in places], axis=0)
    sums = jnp.concatenate([rows10[0:5], rows10[5:10]], axis=1)
    block = jnp.concatenate(list(three_parts(sums)) + [mine], axis=0).astype(BF16)
    for d in range(devices):
        payload[d] = block


def transposed(grad, own_low, w1, wb, x3, stats, features, k1t, params, masks, ws_hbm,
               first, ws, normed_taps, low, g3, rim, sem):
    load = pltpu.make_async_copy(ws_hbm, ws, sem)
    load.start()
    rows = MEL_ROWS
    chan = own_low.shape[0] // rows
    wide = grad.shape[1]
    frame_dev = wide - RIM
    count = grad.shape[0] // chan
    usable = masks[0:1]
    behind, ahead = (masks[n : n + 1].astype(BF16) for n in (1, 2))
    scale = jnp.broadcast_to(stats[chan + 16 :, 0:1], (chan, wide))
    shift = jnp.broadcast_to(stats[chan + 16 :, 1:2], (chan, wide))
    factor = jnp.broadcast_to(to_column(params[0:1], chan) * stats[0:chan, 1:2], (chan, wide))
    edge = (0, 1, 2, 3, count - 4, count - 3, count - 2, count - 1)
    for q in range(count):
        value = grad[q * chan : (q + 1) * chan, :]
        for n, v in enumerate((value,) + shifted_frames(value, behind, ahead)):
            spot = (3 * q + (1, 0, 2)[n]) * chan
            rim[spot : spot + chan, :] = v[:, frame_dev:]
            if q in edge:
                spot = (3 * edge.index(q) + (1, 0, 2)[n]) * chan
                g3[spot : spot + chan, :] = v[:, :frame_dev]
    low[chan : (rows + 1) * chan, :frame_dev] = own_low[...]

    def put(m, lanes, result, pre_one):
        at = slice((m + 1) * chan, (m + 2) * chan)
        _, slope = silu_halves(pre_one * scale[:, lanes] + shift[:, lanes])
        mask = usable[:, lanes] * (0.5 * row_valid(m, rows))
        low[at, lanes] = (result * slope * mask * factor[:, lanes]).astype(BF16)

    pre_one = dot(w1[2 * chan : (rows + 4) * chan, :], x3[:, frame_dev:])
    beside = slice(frame_dev, wide)
    for start in range(0, rows + 2, 2):
        result = dot(wb[...], rim[start * 3 * chan : (start + 4) * 3 * chan, :])
        for n in range(2):
            at = slice((start + n) * chan, (start + n + 1) * chan)
            put(start + n - 1, beside, result[n * chan : (n + 1) * chan], pre_one[at])
    own = slice(0, frame_dev)
    result = dot(wb[...], g3[: 4 * 3 * chan, :])
    put(-1, own, result[:chan], dot(w1[2 * chan : 3 * chan, :], x3[:, :frame_dev]))
    result = dot(wb[...], g3[4 * 3 * chan :, :])
    put(rows, own, result[chan:], dot(w1[(rows + 3) * chan : (rows + 4) * chan, :], x3[:, :frame_dev]))
    row = features[0:1, :]
    lane = iota((1, 128), 1)
    gram = jnp.concatenate(
        [jnp.where(lane < 9, pltpu.roll(row, 128 - 9 * t, 1) if t else row, 0.0) for t in range(9)]
        + [jnp.zeros((7, 128), F32)],
        axis=0,
    )
    single = to_column(row, 16, 81)[0:9]
    k_rows = jnp.concatenate([k1t[...], jnp.zeros((112, chan), F32)], axis=0)
    mean_l, inv_l = stats[chan : chan + 1, :chan], stats[chan + 8 : chan + 9, :chan]
    normed = inv_l * (dot(gram, k_rows, precision=EXACT)[0:9] - single * mean_l)
    normed_taps[0:16] = jnp.concatenate([normed, jnp.zeros((7, chan), F32)], axis=0)
    normed_taps[16:32] = jnp.broadcast_to(to_column(row, 16, 81), (16, chan))
    load.wait()
    first[...] = dot(ws[...], low[...])


def finish(recv, features, stats, k1t, first, ws, w1, x3, normed_taps, params, masks,
           spec_hbm, kernel_one_hbm, kernel_two_hbm, gain_hbm, bias_hbm,
           spec_grad, kernel_one, kernel_two, gain_out, bias_out, got, sems):
    chan = params.shape[1]
    rows = MEL_ROWS
    wide = x3.shape[1]
    frame_dev = wide - RIM
    usable, behind, ahead = (masks[n : n + 1] for n in range(3))
    total = masks[3:4, 0:1]
    gain = params[0:1]
    count = recv.shape[0]
    share = half_share(count, 9 * chan)
    got[...] = recv[...].astype(F32).reshape(count * LAST, 128)
    sums = summed_blocks(got, count)
    sums = sums[0:5] + sums[5:10] + sums[10:15]
    ten = jnp.concatenate([sums[:, :chan], sums[:, chan:]], axis=0)
    bias_sum = ten[9:10]
    mean_l, inv_l = stats[chan : chan + 1, :chan], stats[chan + 8 : chan + 9, :chan]
    ten = ten - features[1:2, 0:1] * bias_sum
    k = k1t[0:9]
    gain_sum = inv_l * (jnp.sum(k * ten[0:9], axis=0, keepdims=True) - mean_l * bias_sum)
    gain_out[...] = gain_sum
    bias_out[...] = bias_sum
    factor_l = gain * inv_l
    scale = factor_l * gain_sum / total * inv_l
    scale = jnp.concatenate(
        [scale * row_valid(-1, rows)] + [scale] * rows + [scale * row_valid(rows, rows)], axis=1
    )
    many = 3 * rows

    def in_parts(v, right):
        high = lax.reduce_precision(v, 8, 7)
        v = dot(jnp.concatenate([high, v - high], axis=0).astype(BF16), right)
        return v[:many] + v[many:]

    combined = in_parts(ws[...].astype(F32) * scale, w1[2 * chan : (rows + 4) * chan, :])
    left = [got[pl.ds(15 + p, count, stride=LAST), :] for p in range(share)]
    taps = TAPS // 2
    whole = [jnp.concatenate([v[:, h * chan : (h + 1) * chan] for v in left], axis=0)[:taps] for h in range(2)]
    whole = jnp.concatenate(whole, axis=0)
    for t in range(9):
        kernel_two[t] = whole[t * chan : (t + 1) * chan].T
    stores = [pltpu.make_async_copy(kernel_two, kernel_two_hbm, sems.at[4])]
    stores[0].start()
    taken = in_parts(combined, x3[...])
    taps = first[...] - taken
    moved = [taps[rows * b : rows * (b + 1)] for b in range(3)]
    mean_full = mean_l + features[1:2, 0:1] * jnp.sum(k, axis=0, keepdims=True)
    constant = jnp.sum(k * (factor_l * (bias_sum - gain_sum * inv_l * mean_full) / total), axis=1, keepdims=True)
    for a in range(3):
        row = iota((rows, 1), 0) + (a - 1) + lax.axis_index("mel") * rows
        valid = ((row >= 0) & (row < lax.axis_size("mel") * rows)).astype(F32) * usable
        for b in range(3):
            t = 3 * (2 - a) + 2 - b
            moved[b] = moved[b] - constant[t : t + 1] * valid
    result = pltpu.roll(moved[0], 1, 1) * behind + moved[1] + pltpu.roll(moved[2], wide - 1, 1) * ahead
    spec_grad[0] = (result * usable)[:, :frame_dev]
    grad_taps = factor_l * (ten[0:9] - (bias_sum * normed_taps[16:25] + gain_sum * normed_taps[0:9]) / total)
    for i in range(3):
        kernel_one[i] = grad_taps[3 * i : 3 * i + 3]
    outs = ((spec_grad, spec_hbm), (kernel_one, kernel_one_hbm), (gain_out, gain_hbm), (bias_out, bias_hbm))
    wait_all(stores + start_all(*outs, sems=sems))


def run(kernel, outs, scratch, *args, hbm=0, apart=(), flops=10**8, size=4 * 10**6):
    vmem = pl.BlockSpec(memory_space=pltpu.VMEM)
    devices = lax.axis_size("mel") * lax.axis_size("tm")
    specs = []
    args = list(args)
    for n, a in enumerate(args):
        if hbm and n >= len(args) - hbm:
            specs.append(pl.BlockSpec(memory_space=pltpu.HBM))
            args[n] = pltpu.with_memory_space_constraint(a, pltpu.HBM)
        else:
            specs.append(vmem)
            args[n] = pltpu.with_memory_space_constraint(a, pltpu.VMEM)
    return pl.pallas_call(
        kernel,
        out_shape=outs,
        in_specs=specs,
        out_specs=[pl.BlockSpec(memory_space=pltpu.HBM) if n in apart else vmem for n in range(len(outs))],
        scratch_shapes=scratch,
        compiler_params=pltpu.CompilerParams(vmem_limit_bytes=(29 + devices // 32) * 2**20),
        cost_estimate=pl.CostEstimate(flops=flops, bytes_accessed=size, transcendentals=0),
    )(*args)


def shape(dims, dtype=F32):
    return jax.ShapeDtypeStruct(dims, dtype)


def kept(dims, dtype=F32):
    return pltpu.VMEM(dims, dtype)


def far(dims, dtype=F32):
    return pltpu.HBM(dims, dtype)


def exchange(blocks, axes=AXES):
    return lax.all_to_all(blocks, axes, 0, 0, tiled=True)


def exchange_rows(rows, axes=AXES):
    return exchange(rows[:, None, :], axes)[:, 0, :]


def shards(spectrum, clip_bounds, kernel_one, gain_one, bias_one, kernel_two, gain_two, bias_two, pooled_grad):
    _, rows, frame_dev = spectrum.shape
    chan = kernel_two.shape[0]
    n_mel, n_tm = lax.axis_size("mel"), lax.axis_size("tm")
    devices = n_mel * n_tm
    half = frame_dev // 2
    wide = frame_dev + RIM
    mels = n_mel * rows

    packed, own, spec, masks = run(
        pack,
        [
            kept((devices, FIRST, 128), BF16),
            kept(pooled_grad.shape, BF16),
            kept(spectrum.shape, BF16),
            kept((8, wide)),
        ],
        [
            pltpu.VMEM(clip_bounds.shape, jnp.int32),
            pltpu.VMEM((2 * chan, half), F32),
            pltpu.VMEM((devices * FIRST, 128), F32),
            pltpu.SemaphoreType.DMA((3,)),
        ],
        spectrum,
        pooled_grad,
        clip_bounds,
        hbm=3,
    )
    recv = exchange(packed)
    ext = rows + 6
    span = 4 * 3 * chan
    wf, wb, w1, ws, pairs, singles, k1t, params, all_masks, edge_masks, twice, own_rows = run(
        weights,
        [
            kept((2 * chan, span), BF16),
            kept((2 * chan, span), BF16),
            kept((ext * chan, 128), BF16),
            far((rows * 3, (rows + 2) * chan), BF16),
            kept((chan, 128)),
            kept((chan, 128)),
            kept((16, chan)),
            kept((8, chan)),
            kept((3 * n_tm, frame_dev)),
            kept((n_tm * 8, 128)),
            kept((128, 128)),
            kept((chan * rows // 2, half), BF16),
        ],
        [
            pltpu.VMEM((9, chan, chan), BF16),
            pltpu.VMEM((3, 3, chan), BF16),
            pltpu.VMEM((4, 1, chan), F32),
            pltpu.VMEM(clip_bounds.shape, jnp.int32),
            pltpu.VMEM((rows * 3, (rows + 2) * chan), BF16),
            pltpu.VMEM((chan * rows // 2, half), F32),
            pltpu.SemaphoreType.DMA((8,)),
        ],
        own,
        clip_bounds,
        jnp.transpose(kernel_two, (2, 3, 0, 1)).reshape(9, chan, chan),
        jnp.transpose(kernel_one, (1, 2, 0)),
        gain_one[None],
        bias_one[None],
        gain_two[None],
        bias_two[None],
        hbm=7,
        apart=(3,),
    )
    pre_two, payload, act, x3, far_rim, stats_one, features = run(
        forward_one,
        [
            kept((rows * chan, wide)),
            kept((devices, SECOND, 128), BF16),
            kept((ext * 3 * chan, wide), BF16),
            kept((128, wide), BF16),
            kept((BAND, RIM)),
            kept((2 * chan + 16, 128)),
            kept((8, 128)),
        ],
        [
            pltpu.VMEM((ext * chan, wide), F32),
            pltpu.VMEM((devices * FIRST, 128), F32),
            pltpu.VMEM((n_tm * 8, 128), F32),
            pltpu.VMEM((mels + 8, RIM), F32),
            pltpu.VMEM((devices * SECOND, 128), F32),
        ],
        recv,
        spec,
        pairs,
        singles,
        twice,
        w1,
        wf,
        params,
        masks,
        all_masks,
        edge_masks,
    )
    recv = exchange(payload)
    grad, kept_half, sent_half, totals, stats_two, row_pairs = run(
        backward_scaled,
        [
            kept((rows * chan, frame_dev)),
            kept((TAPS // 2 + devices, 128)),
            kept((TAPS // 2 + devices, 128)),
            kept((8, 128)),
            kept((chan + 8, 128)),
            kept((rows // 2 * chan, frame_dev)),
        ],
        [
            pltpu.VMEM((rows // 2 * chan, frame_dev), F32),
            pltpu.VMEM((3 * chan + 16, rows * frame_dev), BF16),
            pltpu.VMEM((2, TAPS // 2 + devices, 128), F32),
        ],
        recv,
        pre_two,
        act,
        own_rows,
        params,
        masks,
    )
    received = lax.ppermute(sent_half, "tm", [(i, i ^ 1) for i in range(n_tm)])
    pre_ring, ring, rim = run(
        around,
        [kept((4 * chan, wide)), kept((4 * chan, wide)), kept((rows * chan, RIM))],
        [
            pltpu.VMEM(((rows // 2 + 2) * chan, RIM), F32),
            pltpu.VMEM((2 * chan, frame_dev), F32),
            pltpu.VMEM((devices * SECOND, 128), F32),
            pltpu.VMEM((2 * chan, half), F32),
            pltpu.VMEM((4 * 3 * chan, wide), BF16),
        ],
        recv,
        pre_two,
        act,
        w1,
        wf,
        x3,
        far_rim,
        stats_one,
        masks,
        stats_two,
    )
    (payload,) = run(
        pack_sums,
        [kept((devices * (half_share(devices, 9 * chan) + 2), 128))],
        [],
        kept_half,
        received,
        totals,
        rim,
    )
    recv = exchange_rows(payload)
    grad, own_low, payload, totals = run(
        backward,
        [
            kept(((rows + 4) * chan, wide), BF16),
            kept((rows * chan, frame_dev), BF16),
            kept((devices, LAST, 128), BF16),
            kept((8, 128)),
        ],
        [
            pltpu.VMEM(((rows + 2) * 3 * chan, frame_dev), BF16),
            pltpu.VMEM((rows * chan, frame_dev), F32),
            pltpu.VMEM((rows * chan, 2 * frame_dev), BF16),
        ],
        recv,
        pre_two,
        pre_ring,
        grad,
        ring,
        rim,
        stats_two,
        w1,
        x3,
        stats_one,
        params,
        masks,
        wb,
    )
    recv = exchange(payload)
    pooled, gain_two_grad, bias_two_grad = run(
        pool,
        [shape((1, chan, rows // 2, half), BF16), shape((1, chan)), shape((1, chan))],
        [
            pltpu.VMEM((rows // 2 * chan, 128), F32),
        ],
        totals,
        row_pairs,
    )
    first, ws, normed_taps = run(
        transposed,
        [
            kept((rows * 3, wide)),
            kept((rows * 3, (rows + 2) * chan), BF16),
            kept((32, chan)),
        ],
        [
            pltpu.VMEM(((rows + 2) * chan, wide), BF16),
            pltpu.VMEM((8 * 3 * chan, frame_dev), BF16),
            pltpu.VMEM(((rows + 4) * 3 * chan, RIM), BF16),
            pltpu.SemaphoreType.DMA,
        ],
        grad,
        own_low,
        w1,
        wb,
        x3,
        stats_one,
        features,
        k1t,
        params,
        masks,
        ws,
        hbm=1,
    )
    spec_grad, kernel_one_grad, kernel_two_grad, gain_one_grad, bias_one_grad = run(
        finish,
        [
            shape((1, rows, frame_dev)),
            shape((3, 3, chan)),
            shape((9, chan, chan)),
            shape((1, chan)),
            shape((1, chan)),
        ],
        [
            pltpu.VMEM((1, rows, frame_dev), F32),
            pltpu.VMEM((3, 3, chan), F32),
            pltpu.VMEM((9, chan, chan), F32),
            pltpu.VMEM((1, chan), F32),
            pltpu.VMEM((1, chan), F32),
            pltpu.VMEM((devices * LAST, 128), F32),
            pltpu.SemaphoreType.DMA((5,)),
        ],
        recv,
        features,
        stats_one,
        k1t,
        first,
        ws,
        w1,
        x3,
        normed_taps,
        params,
        masks,
        apart=range(5),
    )
    kernel_two_grad = jnp.transpose(kernel_two_grad.reshape(3, 3, chan, chan), (2, 3, 0, 1))
    return (
        pooled,
        spec_grad,
        jnp.transpose(kernel_one_grad, (2, 0, 1)),
        gain_one_grad[0],
        bias_one_grad[0],
        kernel_two_grad,
        gain_two_grad[0],
        bias_two_grad[0],
    )


def solution(mesh):
    return jax.shard_map(
        shards,
        mesh=mesh,
        in_specs=(
            P(None, "mel", "tm"),
            P(),
            P(),
            P(),
            P(),
            P(),
            P(),
            P(),
            P(None, None, "mel", "tm"),
        ),
        out_specs=(P(None, None, "mel", "tm"), P(None, "mel", "tm"), P(), P(), P(), P(), P(), P()),
        check_vma=False,
    )
```

```python
import math

import jax
import jax.numpy as jnp
from jax import lax
from jax.experimental import pallas as pl
from jax.experimental.pallas import tpu as pltpu
from jax.sharding import PartitionSpec as P

F32 = jnp.float32
BF16 = jnp.bfloat16
AXES = ("mel", "tm")
EXACT = lax.Precision.HIGHEST
RIM = 128
BAND = 24
MEL_ROWS = 16
FIRST = 16
SUMS, EDGES, COLUMNS = 8, 11, 15
SIDE, FAR = 96, 112
FAR_HOLDERS = 32
LAST = 24
TAPS = 576
SECOND = 8


def iota(shape, dim):
    return lax.broadcasted_iota(jnp.int32, shape, dim)


def dot(a, b, over=((1,), (0,)), precision=None):
    return lax.dot_general(a, b, (over, ((), ())), precision=precision, preferred_element_type=F32)


def to_column(lanes, count, start=0):
    shape = (count, lanes.shape[1])
    return jnp.sum(jnp.where(iota(shape, 1) == iota(shape, 0) + start, lanes, 0.0), axis=1, keepdims=True)


def to_lanes(column, start=0, width=128):
    shape = (column.shape[0], width)
    return jnp.sum(jnp.where(iota(shape, 1) == iota(shape, 0) + start, column, 0.0), axis=0, keepdims=True)


def halves(v):
    total = v[:, :128]
    for n in range(128, v.shape[1], 128):
        total = total + v[:, n : n + 128]
    return total


def frame_masks(bounds, frames):
    last = bounds.shape[1] - 1
    end = bounds[:, last:]

    def living(f):
        return (f >= 0) & (f < end)

    def paired(f):
        both = living(f) & living(f + 1)
        for k in range(1, last):
            both = both & (f + 1 != bounds[:, k : k + 1])
        return both

    return tuple(m.astype(F32) for m in (living(frames), paired(frames - 1), paired(frames)))


def row_valid(row, rows):
    mel = lax.axis_index("mel") * rows + row
    return ((mel >= 0) & (mel < lax.axis_size("mel") * rows)).astype(F32)


def start_all(*pairs, sems):
    copies = [pltpu.make_async_copy(src, dst, sems.at[n]) for n, (src, dst) in enumerate(pairs)]
    for copy in copies:
        copy.start()
    return copies


def wait_all(copies):
    for copy in copies:
        copy.wait()


def shifted_frames(value, behind, ahead):
    wide = value.shape[1]
    return pltpu.roll(value, 1, 1) * behind, pltpu.roll(value, wide - 1, 1) * ahead


def three_parts(v):
    high = lax.reduce_precision(v, 8, 7)
    mid = lax.reduce_precision(v - high, 8, 7)
    return high, mid, v - high - mid


def share_of(devices, chan):
    return -(-chan // devices)


def pack(spec_hbm, grad_hbm, bounds_hbm, out, own, spec, masks, bounds, edges, rows_out, sems):
    copies = start_all((bounds_hbm, bounds), (spec_hbm, spec), (grad_hbm, own), sems=sems)
    copies[0].wait()
    wide = masks.shape[1]
    frame_dev = wide - RIM
    devices = out.shape[0]
    rows = MEL_ROWS
    lane = iota((1, wide), 1)
    frames = lax.axis_index("tm") * frame_dev + jnp.where(lane < frame_dev + RIM // 2, lane, lane - wide)
    last = bounds.shape[1] - 1
    pixels = bounds[:, last:].astype(F32) * (lax.axis_size("mel") * rows)
    found = frame_masks(bounds[...], frames)
    masks[...] = jnp.concatenate(
        list(found) + [jnp.full((1, wide), 1.0) * pixels, jnp.zeros((4, wide), F32)], axis=0
    )
    usable, behind, ahead = (m[:, :frame_dev] for m in found)
    copies[1].wait()
    copies[2].wait()
    x = spec[0].astype(F32) * usable
    lane = iota((1, frame_dev), 1)
    row = iota((rows, 1), 0)
    inner = jnp.where((lane > 0) & (lane < frame_dev - 1), usable, 0.0)
    number = (rows - 2) * jnp.sum(inner, axis=1, keepdims=True)
    inner = inner * ((row > 0) & (row < rows - 1)).astype(F32)
    centre = jnp.sum(jnp.sum(x, axis=0, keepdims=True), axis=1, keepdims=True)
    centre = centre / (rows * jnp.maximum(jnp.sum(usable, axis=1, keepdims=True), 1.0))
    centre = lax.reduce_precision(centre, 8, 7)
    shifted = [pltpu.roll(x, 1, 1) * behind, x, pltpu.roll(x, frame_dev - 1, 1) * ahead]
    taps = [pltpu.roll(v, (1 - i) % rows, 0) if i != 1 else v for i in range(3) for v in shifted]
    features = feature_rows(centre, (taps, inner))
    lane = iota((1, 128), 1)
    features = jnp.where(lane == 90, centre, jnp.where(lane == 91, number, features))
    pick = iota((8, frame_dev), 0)
    column = jnp.where(pick < 4, pick, frame_dev - 8 + pick)
    strip = dot((iota((8, frame_dev), 1) == column).astype(BF16), x.astype(BF16), ((1,), (1,)))
    lane = iota((8, 128), 1)
    repeat = (iota((rows, 128), 1) % rows == iota((rows, 128), 0)).astype(BF16)
    strip = jnp.where(lane // rows == iota((8, 128), 0), dot(strip.astype(BF16), repeat), 0.0)
    strip = jnp.sum(strip, axis=0, keepdims=True)

    def put(n, value):
        rows_out[pl.ds(n, devices, stride=FIRST), :] = jnp.broadcast_to(value, (devices, 128))

    near = jnp.concatenate([x[0:2], x[rows - 2 :]], axis=0)
    near = jnp.concatenate([near[:, :128], near[:, 128:]], axis=0)
    for d in range(devices):
        rows_out[FIRST * d : FIRST * d + 8, :] = near
    put(COLUMNS, strip)
    _, chan, many, half = own.shape
    share = share_of(devices, chan)
    holders = chan // share
    g = own[0].astype(F32)
    edges[0:chan] = g[:, 0, :]
    edges[chan:] = g[:, many - 1, :]

    def spread_out(v, held):
        if held < devices:
            v = jnp.concatenate([v, jnp.zeros((devices - held, 128), F32)], axis=0)
        return v

    for n in range(share):
        put(EDGES + n, spread_out(edges[n * holders : (n + 1) * holders, :], holders))
        put(EDGES + share + n, spread_out(edges[chan + n * holders : chan + (n + 1) * holders, :], holders))
    for n in range(2 * share, COLUMNS - EDGES):
        put(EDGES + n, jnp.zeros((1, 128), F32))
    end = iota((8, half), 0)
    at = iota((8, half), 1)
    ends = ((end == 0) & (at == 0)) | ((end == 1) & (at == half - 1))
    columns = dot(ends.astype(BF16), g.reshape(chan * many, half).astype(BF16), ((1,), (1,)))
    group = 128 // many
    source = iota((128, 128), 0)
    lane = iota((group, 128), 1)
    mine = lane // many == iota((group, 128), 0)
    lane8, own8 = iota((8, 128), 1), iota((8, 128), 0)
    parts = three_parts(features)
    for n in range(2):
        side = jnp.zeros((holders, 128), F32)
        for m in range(share):
            move = (iota((128, 128), 1) == SIDE + many * m + source % many).astype(BF16)
            first = m * holders * many // 128
            block = [columns[n : n + 1, 128 * q : 128 * (q + 1)] for q in range(first, first + holders * many // 128)]
            block = jnp.concatenate([jnp.where(mine, v, 0.0) for v in block], axis=0)
            side = side + dot(block.astype(BF16), move)
        far = x[2:4] if n == 0 else x[rows - 4 : rows - 2]
        pieces = [far[r : r + 1, 128 * h : 128 * (h + 1)] for r in range(2) for h in range(2)]
        pieces = jnp.concatenate([jnp.where(lane8 // 16 == own8, v, 0.0) for v in pieces], axis=0)
        far = dot(pieces.astype(BF16), (iota((128, 128), 1) == FAR + source % 16).astype(BF16))
        put(SUMS + n, spread_out(side, holders) + spread_out(far, FAR_HOLDERS) + parts[n])
    put(SUMS + 2, parts[2])
    out[...] = rows_out[...].reshape(out.shape).astype(BF16)


def weights(own, bounds_hbm, k2_hbm, k1_hbm, gain_one_hbm, bias_one_hbm, gain_two_hbm, bias_two_hbm,
            wf, wb, w1, ws_hbm, pairs, singles, k1t, params, all_masks, edge_masks, twice, own_rows,
            k2, k1, vectors, bounds, ws, temp, sems):
    loads = start_all(
        (bounds_hbm, bounds),
        (k2_hbm, k2),
        (k1_hbm, k1),
        (gain_one_hbm, vectors.at[0]),
        (bias_one_hbm, vectors.at[1]),
        (gain_two_hbm, vectors.at[2]),
        (bias_two_hbm, vectors.at[3]),
        sems=sems,
    )
    _, many, count, half = own.shape
    temp[...] = own[0].astype(F32).reshape(many * count, half)
    for r in range(count):
        own_rows[r * many : (r + 1) * many] = temp[pl.ds(r, many, stride=count), :].astype(BF16)
    wait_all(loads)
    chan = k2.shape[1]
    span = wf.shape[1]
    taps = [k2[t].astype(F32) for t in range(9)]
    rest = jnp.zeros((chan, span - 9 * chan), F32)
    forward = jnp.concatenate(taps + [rest], axis=1)
    backward = jnp.concatenate([taps[8 - t].T for t in range(9)] + [rest], axis=1)
    for r in range(wb.shape[0] // chan):
        at = slice(r * chan, (r + 1) * chan)
        wb[at] = (pltpu.roll(backward, 3 * chan * r, 1) if r else backward).astype(BF16)
    full = jnp.concatenate([k1[n].astype(F32) for n in range(3)] + [jnp.zeros((7, chan), F32)], axis=0)
    low = [
        jnp.concatenate([full[3 * (2 - a) + 2 - b : 3 * (2 - a) + 3 - b] for a in range(3)], axis=1)
        for b in range(3)
    ]
    rest = jnp.zeros((1, ws.shape[1] - 3 * chan), F32)
    for b in range(3):
        base = jnp.concatenate([low[b], rest], axis=1)
        many = ws.shape[0] // 3
        rolled = [pltpu.roll(base, chan * m, 1) if m else base for m in range(many)]
        ws[many * b : many * (b + 1)] = jnp.concatenate(rolled, axis=0).astype(BF16)
    store_ws = pltpu.make_async_copy(ws, ws_hbm, sems.at[7])
    store_ws.start()
    count, frame_dev = all_masks.shape[0] // 3, all_masks.shape[1]
    frames = iota((count, frame_dev), 0) * frame_dev + iota((count, frame_dev), 1)
    for n, mask in enumerate(frame_masks(bounds[...], frames)):
        all_masks[n * count : (n + 1) * count] = mask
    q = iota(edge_masks.shape, 0)
    lane = iota(edge_masks.shape, 1)
    k = q % 8
    frames = (q // 8) * frame_dev + jnp.where(k < 4, k, k + frame_dev - 8)
    living, behind, ahead = frame_masks(bounds[...], frames)
    living = jnp.where((k == 0) | (k == 7), living, 0.0)
    edge_masks[...] = jnp.where(lane == 0, living, jnp.where(lane == 1, behind, jnp.where(lane == 2, ahead, 0.0)))
    params[...] = jnp.concatenate(
        [vectors[n] for n in range(4)] + [jnp.zeros((4, chan), F32)], axis=0
    )
    tap = iota((16, 128), 0)
    lane = iota((16, 128), 1)
    i = (tap * 11) >> 5
    ninth = (lane * 57) >> 9
    to_band = (lane == BAND * (tap - 3 * i) + i) & (tap < 9)
    to_left = (ninth == tap) & (tap < 9)
    to_right = (lane - 9 * ninth == tap) & (lane < 81)
    to_single = (lane == 81 + tap) & (tap < 9)
    source = iota((128, 128), 0) - 81
    lane = iota((128, 128), 1)
    ninth = (lane * 57) >> 9
    inside = (source >= 0) & (source < 9) & (lane < 81)
    twice[...] = jnp.where(inside, (source == ninth).astype(F32) + (source == lane - 9 * ninth).astype(F32), 0.0)
    for r in range(wf.shape[0] // chan):
        at = slice(r * chan, (r + 1) * chan)
        wf[at] = (pltpu.roll(forward, 3 * chan * r, 1) if r else forward).astype(BF16)
    k1t[...] = full
    k = full.astype(BF16)
    lanes = [dot(k, select.astype(BF16), ((0,), (0,))) for select in (to_band, to_left, to_right, to_single)]
    pairs[...] = lanes[1] * lanes[2]
    singles[...] = lanes[3]
    for m in range(w1.shape[0] // chan):
        w1[m * chan : (m + 1) * chan] = (pltpu.roll(lanes[0], m, 1) if m else lanes[0]).astype(BF16)
    store_ws.wait()


def feature_rows(centre, *parts):
    def folded(v):
        return jnp.sum(halves(v), axis=0, keepdims=True)

    rows = [jnp.zeros((1, 128), F32)] * 96
    for taps, weight in parts:
        z = [tap - centre for tap in taps]
        for s in range(9):
            left = z[s] * weight
            rows[81 + s] = rows[81 + s] + folded(left)
            for t in range(s, 9):
                rows[9 * s + t] = rows[9 * t + s] = rows[9 * s + t] + folded(left * z[t])
    return to_lanes(jnp.sum(jnp.concatenate(rows, axis=0), axis=1, keepdims=True))


def summed_blocks(ref, devices, by=1):
    block = ref.shape[0] // devices
    period = max(8 // math.gcd(block, 8), by)
    step = period * block
    total = ref[0:step, :]
    for at in range(step, ref.shape[0], step):
        total = total + ref[at : at + step, :]
    results = []
    for first in range(by):
        result = total[first * block : (first + 1) * block]
        for n in range(first + by, period, by):
            result = result + total[n * block : (n + 1) * block]
        results.append(result)
    return results if by > 1 else results[0]


def added(ref, start, stop):
    parts = [ref[d, start:stop].astype(F32) for d in range(ref.shape[0])]
    while len(parts) > 1:
        parts = [a + b for a, b in zip(parts[0::2], parts[1::2])]
    return parts[0]


def moved_rows(v, step):
    if step == 0:
        return v
    count = v.shape[0]
    if abs(step) >= count:
        return jnp.zeros_like(v)
    zero = jnp.zeros((abs(step), v.shape[1]), v.dtype)
    if step > 0:
        return jnp.concatenate([zero, v[: count - step]], axis=0)
    return jnp.concatenate([v[-step:], zero], axis=0)


def silu_halves(h):
    t = jnp.tanh(h)
    one = 1.0 + t
    return h * one, one * (1.0 + h * (1.0 - t))


def act_row(act, r, low, low_masks):
    low = low * low_masks[0]
    chan = low.shape[0]
    for n, v in enumerate((low,) + shifted_frames(low, *low_masks[1:])):
        at = (3 * r + (1, 0, 2)[n]) * chan
        act[at : at + chan, :] = v


def forward_one(recv, spec, pairs, singles, twice, w1, wf, params, masks, all_masks, edge_masks,
                pre_two, payload, act, x3, far_rim, stats, features_out, pre_one, got, strips, halo, rows_out):
    devices = recv.shape[0]
    n_mel, count = lax.axis_size("mel"), lax.axis_size("tm")
    rows = MEL_ROWS
    mels = n_mel * rows
    wide = masks.shape[1]
    frame_dev = wide - RIM
    chan = params.shape[1]
    me_m, me_t = lax.axis_index("mel"), lax.axis_index("tm")
    usable, behind, ahead = (masks[n : n + 1] for n in range(3))
    total = masks[3:4, 0:1]
    got[...] = recv[...].astype(F32).reshape(devices * FIRST, 128)

    def every(n):
        return got[pl.ds(n, devices, stride=FIRST), :]

    lane = iota((count, 128), 1)
    bands = [got[pl.ds(FIRST * k * count + COLUMNS, count, stride=FIRST), :] for k in range(n_mel)]
    for c in range(8):
        column = jnp.zeros((count, 128), F32)
        for k, band in enumerate(bands):
            part = jnp.where(lane // rows == c, band, 0.0)
            column = column + (pltpu.roll(part, rows * (k - c) % 128, 1) if k != c else part)
        strips[pl.ds(c, count, stride=8), :] = column
    at = pl.multiple_of(FIRST * (jnp.maximum(me_m - 1, 0) * count + me_t), 8)
    above = got[pl.ds(at, 8), :] * (me_m > 0).astype(F32)
    at = pl.multiple_of(FIRST * (jnp.minimum(me_m + 1, n_mel - 1) * count + me_t), 8)
    below = got[pl.ds(at, 8), :] * (me_m < n_mel - 1).astype(F32)
    above = jnp.concatenate([above[2:4], above[6:8]], axis=1)
    below = jnp.concatenate([below[0:2], below[4:6]], axis=1)
    own = spec[0].astype(F32) * usable[:, :frame_dev]
    at = pl.multiple_of(8 * jnp.minimum(me_t + 1, count - 1), 8)
    after = strips[pl.ds(at, 8), :][:, :mels] * (me_t + 1 < count).astype(F32)
    at = pl.multiple_of(8 * jnp.maximum(me_t - 1, 0), 8)
    before = strips[pl.ds(at, 8), :][:, :mels] * (me_t > 0).astype(F32)
    sides = jnp.concatenate([after[0:4], before[4:8], jnp.zeros((8, mels), F32)], axis=0).astype(BF16)
    side = iota((16, RIM), 0)
    place = iota((16, RIM), 1) == jnp.where(side < 4, side, jnp.where(side < 8, side + RIM - 8, -1))
    halo[0:8] = jnp.zeros((8, RIM), F32)
    halo[mels : mels + 8] = jnp.zeros((8, RIM), F32)
    halo[4 : mels + 4] = dot(sides, place.astype(BF16), ((0,), (0,)))
    rim = halo[pl.ds(pl.multiple_of(me_m * rows, 8), BAND), :]
    far_rim[...] = rim
    row = iota((BAND, RIM), 0)
    rim = jnp.where((row >= 2) & (row < BAND - 2), rim, 0.0)
    blank = jnp.zeros((2, frame_dev), F32)
    near = jnp.concatenate([jnp.concatenate([blank, above, own, below, blank], axis=0), rim], axis=1)
    x3[...] = jnp.concatenate(
        [
            pltpu.roll(near, 1, 1) * behind,
            near,
            pltpu.roll(near, wide - 1, 1) * ahead,
            jnp.broadcast_to(usable, (BAND, wide)),
            jnp.zeros((128 - 4 * BAND, wide), F32),
        ],
        axis=0,
    ).astype(BF16)
    pre_one[2 * chan : (rows + 4) * chan] = dot(w1[2 * chan : (rows + 4) * chan, :], x3[...])
    lane = iota((1, 128), 1)
    parts = jnp.where(lane < 92, every(SUMS) + every(SUMS + 1) + every(SUMS + 2), 0.0)
    centres, numbers = parts[:, 90:91], parts[:, 91:92]
    centre = jnp.sum(centres * numbers, axis=0, keepdims=True)
    centre = centre / jnp.maximum(jnp.sum(numbers, axis=0, keepdims=True), 1.0)
    delta = centres - centre
    features = jnp.sum(parts + delta * numbers * jnp.where(lane < 81, delta, 1.0), axis=0, keepdims=True)
    moved = jnp.sum(delta * parts, axis=0, keepdims=True)
    def edge_row(k, n):
        first = FIRST * k * count + n
        return jnp.concatenate(
            [got[pl.ds(first, count, stride=FIRST), :], got[pl.ds(first + 4, count, stride=FIRST), :]], axis=1
        )

    edge_rows = [[edge_row(k, n) for n in range(4)] for k in range(n_mel)]
    zero = jnp.zeros((count, frame_dev), F32)
    rows_of = [[], [], []]
    for k, (top, second, fore, bottom) in enumerate(edge_rows):
        for n, v in enumerate((edge_rows[k - 1][3] if k else zero, top, second)):
            rows_of[n].append(v)
        for n, v in enumerate((fore, bottom, edge_rows[k + 1][0] if k + 1 < n_mel else zero)):
            rows_of[n].append(v)
    f_usable, f_behind, f_ahead = (all_masks[n * count : (n + 1) * count, :] for n in range(3))
    lane = iota((count, frame_dev), 1)

    def frame_before(v):
        v = pltpu.roll(v, 1, 1)
        return jnp.where(lane == 0, pltpu.roll(v, 1, 0), v) * f_behind

    def frame_after(v):
        v = pltpu.roll(v, frame_dev - 1, 1)
        return jnp.where(lane == frame_dev - 1, pltpu.roll(v, count - 1, 0), v) * f_ahead

    taps = []
    for group in rows_of:
        for move in (frame_before, lambda v: v, frame_after):
            taps.append(jnp.concatenate([move(v) for v in group], axis=1))
    f_usable = jnp.concatenate([f_usable] * (2 * n_mel), axis=1)
    borders = (taps, f_usable)
    edge = strips[...]
    q_usable, q_behind, q_ahead = (edge_masks[:, n : n + 1] for n in range(3))
    lane = iota((count * 8, 128), 1)
    inside = (lane < mels) & (lane % rows != 0) & (lane % rows != rows - 1)
    shifted = [
        pltpu.roll(edge, 1, 0) * q_behind,
        edge,
        pltpu.roll(edge, count * 8 - 1, 0) * q_ahead,
    ]
    taps = [pltpu.roll(v, (1 - i) % 128, 1) if i != 1 else v for i in range(3) for v in shifted]
    features = features + feature_rows(centre, borders, (taps, jnp.where(inside, q_usable, 0.0)))
    features = jnp.where(iota((1, 128), 1) < 90, features, 0.0)
    near_mean = jnp.sum(singles[...] * features, axis=1, keepdims=True) / total
    around = jnp.sum(singles[...], axis=1, keepdims=True)
    square = jnp.sum(pairs[...] * features, axis=1, keepdims=True)
    square = (square + 2.0 * around * jnp.sum(singles[...] * moved, axis=1, keepdims=True)) / total
    inv = lax.rsqrt(square - near_mean * near_mean + 1e-05)
    mean = near_mean + centre * around
    lane = iota((chan, 128), 1)
    stats[0:chan] = jnp.where(lane == 0, mean, jnp.where(lane == 1, inv, 0.0))
    stats[chan : chan + 8] = jnp.broadcast_to(to_lanes(near_mean), (8, 128))
    stats[chan + 8 : chan + 16] = jnp.broadcast_to(to_lanes(inv), (8, 128))
    scale = 0.5 * to_column(params[0:1], chan) * inv
    shift = 0.5 * to_column(params[1:2], chan) - mean * scale
    stats[chan + 16 :] = jnp.where(lane == 0, scale, jnp.where(lane == 1, shift, 0.0))
    scale = jnp.broadcast_to(scale, (chan, wide))
    shift = jnp.broadcast_to(shift, (chan, wide))
    block, taps = wf.shape
    first = jnp.zeros((chan, 128), F32)
    second = jnp.zeros((chan, 128), F32)
    own_mask = usable[:, :frame_dev]
    low_masks = [m.astype(BF16) for m in (usable, behind, ahead)]
    for r in range(2, rows + 4):
        value, _ = silu_halves(pre_one[r * chan : (r + 1) * chan, :] * scale + shift)
        if not 0 <= r - 3 < rows:
            value = value * row_valid(r - 3, rows)
        act_row(act, r, value.astype(BF16), low_masks)
        if r < 5 or r % 2 == 0:
            continue
        g = (r - 3) // 2
        result = dot(wf[...], act[g * 3 * block : g * 3 * block + taps, :frame_dev])
        at = (g - 1) * block
        pre_two[at : at + block, :frame_dev] = result
        if g % 2 == 0:
            beside = [act[n * 3 * block : n * 3 * block + taps, frame_dev:] for n in (g - 1, g)]
            beside = dot(wf[...], jnp.concatenate(beside, axis=1))
            for n in range(2):
                pre_two[at + (n - 1) * block : at + n * block, frame_dev:] = beside[:, n * RIM : (n + 1) * RIM]
        for q in range(2):
            p = result[q * chan : (q + 1) * chan]
            masked = p * own_mask
            first = first + halves(masked)
            second = second + halves(masked * p)
    moved = dot(jnp.broadcast_to(moved, (8, 128)), twice[...], precision=EXACT)[0:1]
    features_out[...] = jnp.concatenate(
        [features + moved, jnp.broadcast_to(centre, (1, 128)), jnp.zeros((6, 128), F32)], axis=0
    )
    share = share_of(devices, chan)

    def put(n, value):
        rows_out[pl.ds(n, devices, stride=SECOND), :] = jnp.broadcast_to(value, (devices, 128))

    for n in range(share):
        put(3 + n, moved_rows(every(EDGES + share + n), count))
        put(3 + share + n, moved_rows(every(EDGES + n), -count))
    for n in [0, 1, 2] + list(range(3 + 2 * share, SECOND - 1)):
        put(n, jnp.zeros((1, 128), F32))
    lane = iota((devices, 128), 1)
    tm = iota((devices, 128), 0) % count
    at_side = (lane >= SIDE) & (lane < FAR)
    lefts = jnp.where(at_side, every(SUMS), 0.0)
    rights = jnp.where(at_side, every(SUMS + 1), 0.0)
    beside = jnp.zeros((devices, 128), F32)
    for n, step in enumerate((0, count, -count)):
        one = jnp.where(tm > 0, moved_rows(rights, step + 1), 0.0)
        two = jnp.where(tm < count - 1, moved_rows(lefts, step - 1), 0.0)
        beside = beside + pltpu.roll(one, (32 * n - SIDE) % 128, 1) + pltpu.roll(two, (32 * n + 16 - SIDE) % 128, 1)
    outer = jnp.where(lane >= FAR, moved_rows(every(SUMS + 1), count), 0.0)
    beside = beside + pltpu.roll(outer, 128 - 16, 1)
    beside = beside + jnp.where(lane >= FAR, moved_rows(every(SUMS), -count), 0.0)
    put(SECOND - 1, beside)
    first = jnp.sum(first, axis=1, keepdims=True)
    second = jnp.sum(second, axis=1, keepdims=True)
    parts = list(three_parts(to_lanes(first) + to_lanes(second, chan)))
    parts = jnp.concatenate(parts + [jnp.zeros((SECOND - 3, 128), F32)], axis=0)
    for d in range(devices):
        payload[d] = (rows_out[SECOND * d : SECOND * (d + 1), :] + parts).astype(BF16)


def spreading(half):
    lane = iota((half, 2 * half), 1)
    return jnp.where(lane >> 1 == iota((half, 2 * half), 0), 0.25, 0.0).astype(BF16)


def half_share(devices, taps):
    return -(-taps // 2 // devices)


def backward_scaled(recv, pre_two, act, own_rows, params, masks,
                    grad, kept_half, sent_half, totals, stats, pairs, up, right, halved):
    devices = recv.shape[0]
    chan = params.shape[1]
    half = own_rows.shape[1]
    frame_dev = 2 * half
    rows = MEL_ROWS
    up[...] = dot(own_rows[...], spreading(half))
    usable = masks[0:1, :frame_dev]
    total = masks[3:4, 0:1]
    sums = jnp.sum(added(recv, 0, SECOND)[0:3], axis=0, keepdims=True)
    mean = to_column(sums, chan) / total
    inv = lax.rsqrt(to_column(sums, chan, chan) / total - mean * mean + 1e-05)
    scale = 0.5 * to_column(params[2:3], chan) * inv
    shift = 0.5 * to_column(params[3:4], chan) - mean * scale
    lane = iota((chan, 128), 1)
    columns = jnp.zeros((chan, 128), F32)
    for n, column in enumerate((mean, inv, scale, shift)):
        columns = jnp.where(lane == n, column, columns)
    stats[0:chan] = columns
    stats[chan : chan + 8] = jnp.broadcast_to(to_lanes(inv), (8, 128))
    mean, inv, scale, shift = (jnp.broadcast_to(v, (chan, frame_dev)) for v in (mean, inv, scale, shift))
    first = jnp.zeros((chan, 128), F32)
    second = jnp.zeros((chan, 128), F32)
    mask = 0.5 * usable
    right[3 * chan :] = jnp.ones((16, rows * frame_dev), BF16)
    table = jnp.zeros((9 * chan, 3 * chan + 16), F32)
    for m in range(rows):
        at = slice(m * chan, (m + 1) * chan)
        pre = pre_two[at, :frame_dev]
        value, slope = silu_halves(pre * scale + shift)
        value = value * usable
        both = value if m % 2 == 0 else both + value
        if m % 2:
            pairs[m // 2 * chan : (m // 2 + 1) * chan, :] = both
        g = up[m // 2 * chan : (m // 2 + 1) * chan, :] * slope * mask
        grad[at, :] = g
        normed = (pre - mean) * inv
        first = first + halves(g * normed)
        second = second + halves(g)
        lanes = slice(m * frame_dev, (m + 1) * frame_dev)
        right[0:chan, lanes] = g.astype(BF16)
        right[chan : 2 * chan, lanes] = normed.astype(BF16)
        right[2 * chan : 3 * chan, lanes] = (g - right[0:chan, lanes].astype(F32)).astype(BF16)
        if m in (5, 11, rows - 1):
            start = m - m % 6
            left = [act[(n + 2) * 3 * chan : (n + 5) * 3 * chan, :frame_dev] for n in range(start, m + 1)]
            lanes = slice(start * frame_dev, (m + 1) * frame_dev)
            table = table + dot(jnp.concatenate(left, axis=1), right[:, lanes], ((1,), (1,)))
    first = jnp.sum(first, axis=1, keepdims=True)
    second = jnp.sum(second, axis=1, keepdims=True)
    totals[...] = jnp.broadcast_to(to_lanes(first) + to_lanes(second, chan), (8, 128))
    rest = jnp.concatenate([table[:, 2 * chan :], jnp.zeros((9 * chan, chan - 16), F32)], axis=1)
    both = table[:, : 2 * chan] + jnp.where(iota(rest.shape, 1) < chan, rest, 0.0)
    single = rest[:, chan : chan + 1]
    taps = 9 * chan // 2
    lane = iota((devices, 128), 1)
    for h in range(2):
        halved[h, 0:taps] = both[h * taps : (h + 1) * taps]
        constants = jnp.zeros((devices, 128), F32)
        for k in range(half_share(devices, 9 * chan)):
            at = h * taps + k * devices
            ones = single[at : min(at + devices, (h + 1) * taps)]
            if ones.shape[0] < devices:
                ones = jnp.concatenate([ones, jnp.zeros((devices - ones.shape[0], 1), F32)], axis=0)
            constants = jnp.where(lane == k, ones, constants)
        halved[h, taps:] = constants
    core = lax.axis_index("tm") % 2
    kept_half[...] = halved[core]
    sent_half[...] = halved[1 - core]


def around(recv, pre_two, act, w1, wf, x3, far_rim, stats_one, masks, stats, pre_ring, ring, rim,
           sides, up, got, beyond, more):
    devices = recv.shape[0]
    got[...] = recv[:, 0:SECOND, :].astype(F32).reshape(devices * SECOND, 128)
    rows = MEL_ROWS
    many = rows // 2
    wide = pre_two.shape[1]
    frame_dev = wide - RIM
    chan = pre_two.shape[0] // rows
    usable = masks[0:1]
    low_masks = [masks[n : n + 1].astype(BF16) for n in range(3)]
    pieces = got[pl.ds(SECOND - 1, devices, stride=SECOND), :][:FAR_HOLDERS].astype(BF16)
    source = iota((128, 128), 0)
    lane = iota((FAR_HOLDERS, 128), 1)
    mine = lane // 16 == iota((FAR_HOLDERS, 128), 0) % 8
    outer = []
    for first in (SIDE, FAR):
        place = (source - first == iota((128, 128), 1) % 16).astype(BF16)
        v = jnp.where(mine, dot(pieces, place), 0.0)
        v = [jnp.sum(v[8 * n : 8 * n + 8], axis=0, keepdims=True) for n in range(4)]
        outer += [jnp.concatenate(v[2 * r : 2 * r + 2], axis=1) for r in range(2)]
    blank = jnp.zeros((BAND - 4, frame_dev), F32)
    far = jnp.concatenate(outer[:2] + [blank] + outer[2:], axis=0)
    row = iota((BAND, RIM), 0)
    far = jnp.concatenate([far, jnp.where((row < 2) | (row >= BAND - 2), far_rim[...], 0.0)], axis=1)
    far = jnp.concatenate(
        [
            pltpu.roll(far, 1, 1) * masks[1:2],
            far,
            pltpu.roll(far, wide - 1, 1) * masks[2:3],
            jnp.zeros((128 - 3 * BAND, wide), F32),
        ],
        axis=0,
    )
    x_all = (x3[...].astype(F32) + far).astype(BF16)
    scale = jnp.broadcast_to(stats_one[chan + 16 :, 0:1], (chan, wide))
    shift = jnp.broadcast_to(stats_one[chan + 16 :, 1:2], (chan, wide))
    for h, start in enumerate((0, rows + 4)):
        pre_one = dot(w1[start * chan : (start + 2) * chan, :], x_all)
        for n in range(2):
            value, _ = silu_halves(pre_one[n * chan : (n + 1) * chan] * scale + shift)
            value = value * row_valid(start + n - 3, rows)
            act_row(more, 2 * h + n, value.astype(BF16), low_masks)
    line = 3 * chan
    above = jnp.concatenate([more[0 : 2 * line, :], act[2 * line : 4 * line, :]], axis=0)
    below = jnp.concatenate([act[(rows + 2) * line : (rows + 4) * line, :], more[2 * line :, :]], axis=0)
    pre_ring[0 : 2 * chan] = dot(wf[...], above)
    pre_ring[2 * chan :] = dot(wf[...], below)
    share = share_of(devices, chan)
    holders = chan // share

    def every(n):
        return got[pl.ds(n, devices, stride=SECOND), :]

    beside = 0.25 * every(SECOND - 1)[:holders]
    lane = iota((holders, RIM), 1)
    for n in range(share):
        first = n * holders
        beyond[first : first + holders, :] = every(3 + n)[:holders]
        beyond[chan + first : chan + first + holders, :] = every(3 + share + n)[:holders]
        for r in range(many + 2):
            at = many * n + (r if r < many else 32 + many - 1 if r == many else 64)
            left, right_of = beside[:, at : at + 1], beside[:, at + 16 : at + 17]
            side = jnp.where(lane >= RIM - 2, left, jnp.where(lane < 2, right_of, 0.0))
            sides[r * chan + first : r * chan + first + holders, :] = side
    up[...] = dot(beyond[...].astype(BF16), spreading(frame_dev // 2))
    scale = jnp.broadcast_to(stats[0:chan, 2:3], (chan, wide))
    shift = jnp.broadcast_to(stats[0:chan, 3:4], (chan, wide))
    for n, m in enumerate((-2, -1, rows, rows + 1)):
        below = n // 2
        upstream = jnp.concatenate(
            [
                up[below * chan : (below + 1) * chan, :],
                sides[(many + below) * chan : (many + below + 1) * chan, :],
            ],
            axis=1,
        )
        _, slope = silu_halves(pre_ring[n * chan : (n + 1) * chan, :] * scale + shift)
        ring[n * chan : (n + 1) * chan, :] = upstream * slope * (usable * (0.5 * row_valid(m, rows)))
    for m in range(rows):
        at = slice(m * chan, (m + 1) * chan)
        _, slope = silu_halves(pre_two[at, frame_dev:] * scale[:, frame_dev:] + shift[:, frame_dev:])
        upstream = sides[m // 2 * chan : (m // 2 + 1) * chan, :]
        rim[m * chan : (m + 1) * chan, :] = upstream * slope * (0.5 * usable[:, frame_dev:])


def pack_sums(kept_half, received, totals, after, payload):
    del after
    devices = kept_half.shape[0] - TAPS // 2
    block = payload.shape[0] // devices
    payload[pl.ds(0, devices, stride=block), :] = jnp.broadcast_to(totals[0:1], (devices, 128))
    taps = TAPS // 2
    total = kept_half[...] + received[...]
    for k in range(block - 2):
        cut = total[k * devices : min((k + 1) * devices, taps)]
        if cut.shape[0] < devices:
            cut = jnp.concatenate([cut, jnp.zeros((devices - cut.shape[0], 128), F32)], axis=0)
        payload[pl.ds(1 + k, devices, stride=block), :] = cut
    payload[pl.ds(block - 1, devices, stride=block), :] = total[taps:]


def pool(totals, pairs, out, gain_out, bias_out, temp):
    gain_out[...] = totals[0:1, : gain_out.shape[1]]
    bias_out[...] = totals[0:1, gain_out.shape[1] :]
    chan, rows, half = out.shape[1:]
    to_mean = jnp.where(iota((2 * half, half), 0) >> 1 == iota((2 * half, half), 1), 0.25, 0.0)
    pooled = dot(pairs[...], to_mean, precision=EXACT)
    for r in range(rows):
        temp[pl.ds(r, chan, stride=rows), :] = pooled[r * chan : (r + 1) * chan]
    out[0] = temp[...].reshape(chan, rows, half).astype(BF16)


def backward(recv, pre_two, pre_ring, grad, ring, rim, stats_two, w1, x3, stats, params, masks, wb,
             out, own_low, payload, totals, g3, pre_one, g1):
    chan = params.shape[1]
    rows = MEL_ROWS
    wide = pre_two.shape[1]
    frame_dev = wide - RIM
    usable = masks[0:1]
    behind, ahead = (masks[n : n + 1].astype(BF16) for n in (1, 2))
    total = masks[3:4, 0:1]
    devices = payload.shape[0]
    pre_one[...] = dot(w1[3 * chan : (rows + 3) * chan], x3[:, :frame_dev])

    even, odd = summed_blocks(recv, devices, 2)
    sums = even[0:1] + odd[0:1]
    gain_sum, bias_sum = sums[:, :chan], sums[:, chan:]
    totals[...] = jnp.broadcast_to(sums, (8, 128))
    mean, inv = stats_two[0:chan, 0:1], stats_two[0:chan, 1:2]
    factor = to_column(params[2:3], chan) * inv
    gain_part = factor * (to_column(sums, chan) / total * inv)
    bias_part = factor * (to_column(sums, chan, chan) / total) - mean * gain_part
    gain_part = jnp.broadcast_to(gain_part, (chan, wide))
    bias_part = jnp.broadcast_to(bias_part, (chan, wide))
    factor = jnp.broadcast_to(factor, (chan, wide))
    scale = jnp.broadcast_to(stats[chan + 16 :, 0:1], (chan, frame_dev))
    shift = jnp.broadcast_to(stats[chan + 16 :, 1:2], (chan, frame_dev))
    factor_one = jnp.broadcast_to(to_column(params[0:1], chan) * stats[0:chan, 1:2], (chan, frame_dev))
    own_mask = 0.5 * usable[:, :frame_dev]
    count = rows + 4
    share = even.shape[0] - 2
    mine = jnp.concatenate([even[1 : share + 1], odd[1 : share + 1]], axis=0)
    single = jnp.concatenate([to_column(v[share + 1 :], share) for v in (even, odd)], axis=0)
    factor_l = params[2:3] * stats_two[chan : chan + 1, :chan]
    mine = mine[:, :chan] - (bias_sum * single + gain_sum * mine[:, chan:]) / total
    mine = factor_l * mine
    mine = jnp.concatenate([mine[:share], mine[share:]], axis=1)
    if share < 9:
        mine = jnp.concatenate([mine, jnp.zeros((9 - share, 128), F32)], axis=0)
    table = jnp.zeros((chan, 128), F32)

    def tap_sums(m):
        taps_in = jnp.concatenate([x3[:, :frame_dev]] * 2, axis=1)
        products = dot(g1[m * chan : (m + 4) * chan, :], taps_in, ((1,), (1,)))
        moved = [pltpu.roll(products[k * chan : (k + 1) * chan], 128 - (m + k + 3), 1) for k in range(4)]
        return (moved[0] + moved[1]) + (moved[2] + moved[3])

    for q in range(count):
        at = slice(q * chan, (q + 1) * chan)
        mask = usable if 0 <= q - 2 < rows else usable * row_valid(q - 2, rows)
        if 2 <= q < rows + 2:
            own = slice((q - 2) * chan, (q - 1) * chan)
            pre, scaled = pre_two[own, :], jnp.concatenate([grad[own, :], rim[own, :]], axis=1)
        else:
            n = q if q < 2 else q - rows
            pre, scaled = pre_ring[n * chan : (n + 1) * chan, :], ring[n * chan : (n + 1) * chan, :]
        low = (factor * scaled - (bias_part + pre * gain_part) * mask).astype(BF16)
        out[at, :] = low
        if not 1 <= q < count - 1:
            continue
        base = (q - 1) * 3 * chan
        for n, v in enumerate((low,) + shifted_frames(low, behind, ahead)):
            spot = base + (1, 0, 2)[n] * chan
            g3[spot : spot + chan, :] = v[:, :frame_dev]
        start = q - 4
        if start < 0 or start % 2:
            continue
        result = dot(wb[...], g3[start * 3 * chan : (start + 4) * 3 * chan, :])
        for n in range(2):
            m = start + n
            at = slice(m * chan, (m + 1) * chan)
            _, slope = silu_halves(pre_one[at, :] * scale + shift)
            value = result[n * chan : (n + 1) * chan] * slope * own_mask
            own_low[at, :] = (value * factor_one).astype(BF16)
            g1[at, :frame_dev] = value.astype(BF16)
            g1[at, frame_dev:] = (value - g1[at, :frame_dev].astype(F32)).astype(BF16)
        if start % 4 == 2 and start > 2:
            table = table + tap_sums(start - 6)
    table = table + tap_sums(rows - 4)
    table = table.T
    places = [BAND * j + i for i in range(3) for j in range(3)] + [3 * BAND]
    rows10 = jnp.concatenate([table[n : n + 1] for n in places], axis=0)
    sums = jnp.concatenate([rows10[0:5], rows10[5:10]], axis=1)
    block = jnp.concatenate(list(three_parts(sums)) + [mine], axis=0).astype(BF16)
    for d in range(devices):
        payload[d] = block


def transposed(grad, own_low, w1, wb, x3, stats, features, k1t, params, masks, ws_hbm,
               first, ws, normed_taps, low, g3, rim, sem):
    load = pltpu.make_async_copy(ws_hbm, ws, sem)
    load.start()
    rows = MEL_ROWS
    chan = own_low.shape[0] // rows
    wide = grad.shape[1]
    frame_dev = wide - RIM
    count = grad.shape[0] // chan
    usable = masks[0:1]
    behind, ahead = (masks[n : n + 1].astype(BF16) for n in (1, 2))
    scale = jnp.broadcast_to(stats[chan + 16 :, 0:1], (chan, wide))
    shift = jnp.broadcast_to(stats[chan + 16 :, 1:2], (chan, wide))
    factor = jnp.broadcast_to(to_column(params[0:1], chan) * stats[0:chan, 1:2], (chan, wide))
    edge = (0, 1, 2, 3, count - 4, count - 3, count - 2, count - 1)
    for q in range(count):
        value = grad[q * chan : (q + 1) * chan, :]
        for n, v in enumerate((value,) + shifted_frames(value, behind, ahead)):
            spot = (3 * q + (1, 0, 2)[n]) * chan
            rim[spot : spot + chan, :] = v[:, frame_dev:]
            if q in edge:
                spot = (3 * edge.index(q) + (1, 0, 2)[n]) * chan
                g3[spot : spot + chan, :] = v[:, :frame_dev]
    low[chan : (rows + 1) * chan, :frame_dev] = own_low[...]

    def put(m, lanes, result, pre_one):
        at = slice((m + 1) * chan, (m + 2) * chan)
        _, slope = silu_halves(pre_one * scale[:, lanes] + shift[:, lanes])
        mask = usable[:, lanes] * (0.5 * row_valid(m, rows))
        low[at, lanes] = (result * slope * mask * factor[:, lanes]).astype(BF16)

    pre_one = dot(w1[2 * chan : (rows + 4) * chan, :], x3[:, frame_dev:])
    beside = slice(frame_dev, wide)
    for start in range(0, rows + 2, 2):
        result = dot(wb[...], rim[start * 3 * chan : (start + 4) * 3 * chan, :])
        for n in range(2):
            at = slice((start + n) * chan, (start + n + 1) * chan)
            put(start + n - 1, beside, result[n * chan : (n + 1) * chan], pre_one[at])
    own = slice(0, frame_dev)
    result = dot(wb[...], g3[: 4 * 3 * chan, :])
    put(-1, own, result[:chan], dot(w1[2 * chan : 3 * chan, :], x3[:, :frame_dev]))
    result = dot(wb[...], g3[4 * 3 * chan :, :])
    put(rows, own, result[chan:], dot(w1[(rows + 3) * chan : (rows + 4) * chan, :], x3[:, :frame_dev]))
    row = features[0:1, :]
    lane = iota((1, 128), 1)
    gram = jnp.concatenate(
        [jnp.where(lane < 9, pltpu.roll(row, 128 - 9 * t, 1) if t else row, 0.0) for t in range(9)]
        + [jnp.zeros((7, 128), F32)],
        axis=0,
    )
    single = to_column(row, 16, 81)[0:9]
    k_rows = jnp.concatenate([k1t[...], jnp.zeros((112, chan), F32)], axis=0)
    mean_l, inv_l = stats[chan : chan + 1, :chan], stats[chan + 8 : chan + 9, :chan]
    normed = inv_l * (dot(gram, k_rows, precision=EXACT)[0:9] - single * mean_l)
    normed_taps[0:16] = jnp.concatenate([normed, jnp.zeros((7, chan), F32)], axis=0)
    normed_taps[16:32] = jnp.broadcast_to(to_column(row, 16, 81), (16, chan))
    load.wait()
    first[...] = dot(ws[...], low[...])


def finish(recv, features, stats, k1t, first, ws, w1, x3, normed_taps, params, masks,
           spec_hbm, kernel_one_hbm, kernel_two_hbm, gain_hbm, bias_hbm,
           spec_grad, kernel_one, kernel_two, gain_out, bias_out, got, sems):
    chan = params.shape[1]
    rows = MEL_ROWS
    wide = x3.shape[1]
    frame_dev = wide - RIM
    usable, behind, ahead = (masks[n : n + 1] for n in range(3))
    total = masks[3:4, 0:1]
    gain = params[0:1]
    count = recv.shape[0]
    share = half_share(count, 9 * chan)
    sums = added(recv, 0, 16)
    sums = sums[0:5] + sums[5:10] + sums[10:15]
    ten = jnp.concatenate([sums[:, :chan], sums[:, chan:]], axis=0)
    bias_sum = ten[9:10]
    mean_l, inv_l = stats[chan : chan + 1, :chan], stats[chan + 8 : chan + 9, :chan]
    ten = ten - features[1:2, 0:1] * bias_sum
    k = k1t[0:9]
    gain_sum = inv_l * (jnp.sum(k * ten[0:9], axis=0, keepdims=True) - mean_l * bias_sum)
    gain_out[...] = gain_sum
    bias_out[...] = bias_sum
    factor_l = gain * inv_l
    scale = factor_l * gain_sum / total * inv_l
    scale = jnp.concatenate(
        [scale * row_valid(-1, rows)] + [scale] * rows + [scale * row_valid(rows, rows)], axis=1
    )
    many = 3 * rows

    def in_parts(v, right):
        high = lax.reduce_precision(v, 8, 7)
        v = dot(jnp.concatenate([high, v - high], axis=0).astype(BF16), right)
        return v[:many] + v[many:]

    combined = in_parts(ws[...].astype(F32) * scale, w1[2 * chan : (rows + 4) * chan, :])
    got[...] = recv[...].astype(F32).reshape(count * LAST, 128)
    left = [got[pl.ds(15 + p, count, stride=LAST), :] for p in range(share)]
    taps = TAPS // 2
    whole = [jnp.concatenate([v[:, h * chan : (h + 1) * chan] for v in left], axis=0)[:taps] for h in range(2)]
    whole = jnp.concatenate(whole, axis=0)
    for t in range(9):
        kernel_two[t] = whole[t * chan : (t + 1) * chan].T
    stores = [pltpu.make_async_copy(kernel_two, kernel_two_hbm, sems.at[4])]
    stores[0].start()
    taken = in_parts(combined, x3[...])
    taps = first[...] - taken
    moved = [taps[rows * b : rows * (b + 1)] for b in range(3)]
    mean_full = mean_l + features[1:2, 0:1] * jnp.sum(k, axis=0, keepdims=True)
    constant = jnp.sum(k * (factor_l * (bias_sum - gain_sum * inv_l * mean_full) / total), axis=1, keepdims=True)
    for a in range(3):
        row = iota((rows, 1), 0) + (a - 1) + lax.axis_index("mel") * rows
        valid = ((row >= 0) & (row < lax.axis_size("mel") * rows)).astype(F32) * usable
        for b in range(3):
            t = 3 * (2 - a) + 2 - b
            moved[b] = moved[b] - constant[t : t + 1] * valid
    result = pltpu.roll(moved[0], 1, 1) * behind + moved[1] + pltpu.roll(moved[2], wide - 1, 1) * ahead
    spec_grad[0] = (result * usable)[:, :frame_dev]
    grad_taps = factor_l * (ten[0:9] - (bias_sum * normed_taps[16:25] + gain_sum * normed_taps[0:9]) / total)
    for i in range(3):
        kernel_one[i] = grad_taps[3 * i : 3 * i + 3]
    outs = ((spec_grad, spec_hbm), (kernel_one, kernel_one_hbm), (gain_out, gain_hbm), (bias_out, bias_hbm))
    wait_all(stores + start_all(*outs, sems=sems))


def run(kernel, outs, scratch, *args, hbm=0, apart=(), flops=10**8, size=4 * 10**6):
    vmem = pl.BlockSpec(memory_space=pltpu.VMEM)
    devices = lax.axis_size("mel") * lax.axis_size("tm")
    specs = []
    args = list(args)
    for n, a in enumerate(args):
        if hbm and n >= len(args) - hbm:
            specs.append(pl.BlockSpec(memory_space=pltpu.HBM))
            args[n] = pltpu.with_memory_space_constraint(a, pltpu.HBM)
        else:
            specs.append(vmem)
            args[n] = pltpu.with_memory_space_constraint(a, pltpu.VMEM)
    return pl.pallas_call(
        kernel,
        out_shape=outs,
        in_specs=specs,
        out_specs=[pl.BlockSpec(memory_space=pltpu.HBM) if n in apart else vmem for n in range(len(outs))],
        scratch_shapes=scratch,
        compiler_params=pltpu.CompilerParams(vmem_limit_bytes=(29 + devices // 32) * 2**20),
        cost_estimate=pl.CostEstimate(flops=flops, bytes_accessed=size, transcendentals=0),
    )(*args)


def shape(dims, dtype=F32):
    return jax.ShapeDtypeStruct(dims, dtype)


def kept(dims, dtype=F32):
    return pltpu.VMEM(dims, dtype)


def far(dims, dtype=F32):
    return pltpu.HBM(dims, dtype)


def exchange(blocks, axes=AXES):
    return lax.all_to_all(blocks, axes, 0, 0, tiled=True)


def exchange_rows(rows, axes=AXES):
    return exchange(rows[:, None, :], axes)[:, 0, :]


def shards(spectrum, clip_bounds, kernel_one, gain_one, bias_one, kernel_two, gain_two, bias_two, pooled_grad):
    _, rows, frame_dev = spectrum.shape
    chan = kernel_two.shape[0]
    n_mel, n_tm = lax.axis_size("mel"), lax.axis_size("tm")
    devices = n_mel * n_tm
    half = frame_dev // 2
    wide = frame_dev + RIM
    mels = n_mel * rows

    packed, own, spec, masks = run(
        pack,
        [
            kept((devices, FIRST, 128), BF16),
            kept(pooled_grad.shape, BF16),
            kept(spectrum.shape, BF16),
            kept((8, wide)),
        ],
        [
            pltpu.VMEM(clip_bounds.shape, jnp.int32),
            pltpu.VMEM((2 * chan, half), F32),
            pltpu.VMEM((devices * FIRST, 128), F32),
            pltpu.SemaphoreType.DMA((3,)),
        ],
        spectrum,
        pooled_grad,
        clip_bounds,
        hbm=3,
    )
    recv = exchange(packed)
    ext = rows + 6
    span = 4 * 3 * chan
    wf, wb, w1, ws, pairs, singles, k1t, params, all_masks, edge_masks, twice, own_rows = run(
        weights,
        [
            kept((2 * chan, span), BF16),
            kept((2 * chan, span), BF16),
            kept((ext * chan, 128), BF16),
            far((rows * 3, (rows + 2) * chan), BF16),
            kept((chan, 128)),
            kept((chan, 128)),
            kept((16, chan)),
            kept((8, chan)),
            kept((3 * n_tm, frame_dev)),
            kept((n_tm * 8, 128)),
            kept((128, 128)),
            kept((chan * rows // 2, half), BF16),
        ],
        [
            pltpu.VMEM((9, chan, chan), BF16),
            pltpu.VMEM((3, 3, chan), BF16),
            pltpu.VMEM((4, 1, chan), F32),
            pltpu.VMEM(clip_bounds.shape, jnp.int32),
            pltpu.VMEM((rows * 3, (rows + 2) * chan), BF16),
            pltpu.VMEM((chan * rows // 2, half), F32),
            pltpu.SemaphoreType.DMA((8,)),
        ],
        own,
        clip_bounds,
        jnp.transpose(kernel_two, (2, 3, 0, 1)).reshape(9, chan, chan),
        jnp.transpose(kernel_one, (1, 2, 0)),
        gain_one[None],
        bias_one[None],
        gain_two[None],
        bias_two[None],
        hbm=7,
        apart=(3,),
    )
    pre_two, payload, act, x3, far_rim, stats_one, features = run(
        forward_one,
        [
            kept((rows * chan, wide)),
            kept((devices, SECOND, 128), BF16),
            kept((ext * 3 * chan, wide), BF16),
            kept((128, wide), BF16),
            kept((BAND, RIM)),
            kept((2 * chan + 16, 128)),
            kept((8, 128)),
        ],
        [
            pltpu.VMEM((ext * chan, wide), F32),
            pltpu.VMEM((devices * FIRST, 128), F32),
            pltpu.VMEM((n_tm * 8, 128), F32),
            pltpu.VMEM((mels + 8, RIM), F32),
            pltpu.VMEM((devices * SECOND, 128), F32),
        ],
        recv,
        spec,
        pairs,
        singles,
        twice,
        w1,
        wf,
        params,
        masks,
        all_masks,
        edge_masks,
    )
    recv = exchange(payload)
    grad, kept_half, sent_half, totals, stats_two, row_pairs = run(
        backward_scaled,
        [
            kept((rows * chan, frame_dev)),
            kept((TAPS // 2 + devices, 128)),
            kept((TAPS // 2 + devices, 128)),
            kept((8, 128)),
            kept((chan + 8, 128)),
            kept((rows // 2 * chan, frame_dev)),
        ],
        [
            pltpu.VMEM((rows // 2 * chan, frame_dev), F32),
            pltpu.VMEM((3 * chan + 16, rows * frame_dev), BF16),
            pltpu.VMEM((2, TAPS // 2 + devices, 128), F32),
        ],
        recv,
        pre_two,
        act,
        own_rows,
        params,
        masks,
    )
    received = lax.ppermute(sent_half, "tm", [(i, i ^ 1) for i in range(n_tm)])
    pre_ring, ring, rim = run(
        around,
        [kept((4 * chan, wide)), kept((4 * chan, wide)), kept((rows * chan, RIM))],
        [
            pltpu.VMEM(((rows // 2 + 2) * chan, RIM), F32),
            pltpu.VMEM((2 * chan, frame_dev), F32),
            pltpu.VMEM((devices * SECOND, 128), F32),
            pltpu.VMEM((2 * chan, half), F32),
            pltpu.VMEM((4 * 3 * chan, wide), BF16),
        ],
        recv,
        pre_two,
        act,
        w1,
        wf,
        x3,
        far_rim,
        stats_one,
        masks,
        stats_two,
    )
    (payload,) = run(
        pack_sums,
        [kept((devices * (half_share(devices, 9 * chan) + 2), 128))],
        [],
        kept_half,
        received,
        totals,
        rim,
    )
    recv = exchange_rows(payload)
    grad, own_low, payload, totals = run(
        backward,
        [
            kept(((rows + 4) * chan, wide), BF16),
            kept((rows * chan, frame_dev), BF16),
            kept((devices, LAST, 128), BF16),
            kept((8, 128)),
        ],
        [
            pltpu.VMEM(((rows + 2) * 3 * chan, frame_dev), BF16),
            pltpu.VMEM((rows * chan, frame_dev), F32),
            pltpu.VMEM((rows * chan, 2 * frame_dev), BF16),
        ],
        recv,
        pre_two,
        pre_ring,
        grad,
        ring,
        rim,
        stats_two,
        w1,
        x3,
        stats_one,
        params,
        masks,
        wb,
    )
    recv = exchange(payload)
    pooled, gain_two_grad, bias_two_grad = run(
        pool,
        [shape((1, chan, rows // 2, half), BF16), shape((1, chan)), shape((1, chan))],
        [
            pltpu.VMEM((rows // 2 * chan, 128), F32),
        ],
        totals,
        row_pairs,
    )
    first, ws, normed_taps = run(
        transposed,
        [
            kept((rows * 3, wide)),
            kept((rows * 3, (rows + 2) * chan), BF16),
            kept((32, chan)),
        ],
        [
            pltpu.VMEM(((rows + 2) * chan, wide), BF16),
            pltpu.VMEM((8 * 3 * chan, frame_dev), BF16),
            pltpu.VMEM(((rows + 4) * 3 * chan, RIM), BF16),
            pltpu.SemaphoreType.DMA,
        ],
        grad,
        own_low,
        w1,
        wb,
        x3,
        stats_one,
        features,
        k1t,
        params,
        masks,
        ws,
        hbm=1,
    )
    spec_grad, kernel_one_grad, kernel_two_grad, gain_one_grad, bias_one_grad = run(
        finish,
        [
            shape((1, rows, frame_dev)),
            shape((3, 3, chan)),
            shape((9, chan, chan)),
            shape((1, chan)),
            shape((1, chan)),
        ],
        [
            pltpu.VMEM((1, rows, frame_dev), F32),
            pltpu.VMEM((3, 3, chan), F32),
            pltpu.VMEM((9, chan, chan), F32),
            pltpu.VMEM((1, chan), F32),
            pltpu.VMEM((1, chan), F32),
            pltpu.VMEM((devices * LAST, 128), F32),
            pltpu.SemaphoreType.DMA((5,)),
        ],
        recv,
        features,
        stats_one,
        k1t,
        first,
        ws,
        w1,
        x3,
        normed_taps,
        params,
        masks,
        apart=range(5),
    )
    kernel_two_grad = jnp.transpose(kernel_two_grad.reshape(3, 3, chan, chan), (2, 3, 0, 1))
    return (
        pooled,
        spec_grad,
        jnp.transpose(kernel_one_grad, (2, 0, 1)),
        gain_one_grad[0],
        bias_one_grad[0],
        kernel_two_grad,
        gain_two_grad[0],
        bias_two_grad[0],
    )


def solution(mesh):
    return jax.shard_map(
        shards,
        mesh=mesh,
        in_specs=(
            P(None, "mel", "tm"),
            P(),
            P(),
            P(),
            P(),
            P(),
            P(),
            P(),
            P(None, None, "mel", "tm"),
        ),
        out_specs=(P(None, None, "mel", "tm"), P(None, "mel", "tm"), P(), P(), P(), P(), P(), P()),
        check_vma=False,
    )
```

```python
import math

import jax
import jax.numpy as jnp
from jax import lax
from jax.experimental import pallas as pl
from jax.experimental.pallas import tpu as pltpu
from jax.sharding import PartitionSpec as P

F32 = jnp.float32
BF16 = jnp.bfloat16
AXES = ("mel", "tm")
EXACT = lax.Precision.HIGHEST
RIM = 128
BAND = 24
MEL_ROWS = 16
FIRST = 16
SUMS, EDGES, COLUMNS = 8, 11, 15
SIDE, FAR = 96, 112
FAR_HOLDERS = 32
LAST = 24
TAPS = 576
SECOND = 8


def iota(shape, dim):
    return lax.broadcasted_iota(jnp.int32, shape, dim)


def dot(a, b, over=((1,), (0,)), precision=None):
    return lax.dot_general(a, b, (over, ((), ())), precision=precision, preferred_element_type=F32)


def to_column(lanes, count, start=0):
    shape = (count, lanes.shape[1])
    return jnp.sum(jnp.where(iota(shape, 1) == iota(shape, 0) + start, lanes, 0.0), axis=1, keepdims=True)


def to_lanes(column, start=0, width=128):
    shape = (column.shape[0], width)
    return jnp.sum(jnp.where(iota(shape, 1) == iota(shape, 0) + start, column, 0.0), axis=0, keepdims=True)


def halves(v):
    total = v[:, :128]
    for n in range(128, v.shape[1], 128):
        total = total + v[:, n : n + 128]
    return total


def frame_masks(bounds, frames):
    last = bounds.shape[1] - 1
    end = bounds[:, last:]

    def living(f):
        return (f >= 0) & (f < end)

    def paired(f):
        both = living(f) & living(f + 1)
        for k in range(1, last):
            both = both & (f + 1 != bounds[:, k : k + 1])
        return both

    return tuple(m.astype(F32) for m in (living(frames), paired(frames - 1), paired(frames)))


def row_valid(row, rows):
    mel = lax.axis_index("mel") * rows + row
    return ((mel >= 0) & (mel < lax.axis_size("mel") * rows)).astype(F32)


def start_all(*pairs, sems):
    copies = [pltpu.make_async_copy(src, dst, sems.at[n]) for n, (src, dst) in enumerate(pairs)]
    for copy in copies:
        copy.start()
    return copies


def wait_all(copies):
    for copy in copies:
        copy.wait()


def shifted_frames(value, behind, ahead):
    wide = value.shape[1]
    return pltpu.roll(value, 1, 1) * behind, pltpu.roll(value, wide - 1, 1) * ahead


def three_parts(v):
    high = lax.reduce_precision(v, 8, 7)
    mid = lax.reduce_precision(v - high, 8, 7)
    return high, mid, v - high - mid


def share_of(devices, chan):
    return -(-chan // devices)


def pack(spec_hbm, grad_hbm, bounds_hbm, out, own, spec, masks, bounds, edges, rows_out, sems):
    copies = start_all((bounds_hbm, bounds), (spec_hbm, spec), (grad_hbm, own), sems=sems)
    copies[0].wait()
    wide = masks.shape[1]
    frame_dev = wide - RIM
    devices = out.shape[0]
    rows = MEL_ROWS
    lane = iota((1, wide), 1)
    frames = lax.axis_index("tm") * frame_dev + jnp.where(lane < frame_dev + RIM // 2, lane, lane - wide)
    last = bounds.shape[1] - 1
    pixels = bounds[:, last:].astype(F32) * (lax.axis_size("mel") * rows)
    found = frame_masks(bounds[...], frames)
    masks[...] = jnp.concatenate(
        list(found) + [jnp.full((1, wide), 1.0) * pixels, jnp.zeros((4, wide), F32)], axis=0
    )
    usable, behind, ahead = (m[:, :frame_dev] for m in found)
    copies[1].wait()
    x = spec[0].astype(F32) * usable
    lane = iota((1, frame_dev), 1)
    row = iota((rows, 1), 0)
    inner = jnp.where((lane > 0) & (lane < frame_dev - 1), usable, 0.0)
    number = (rows - 2) * jnp.sum(inner, axis=1, keepdims=True)
    inner = inner * ((row > 0) & (row < rows - 1)).astype(F32)
    centre = jnp.sum(jnp.sum(x, axis=0, keepdims=True), axis=1, keepdims=True)
    centre = centre / (rows * jnp.maximum(jnp.sum(usable, axis=1, keepdims=True), 1.0))
    centre = lax.reduce_precision(centre, 8, 7)
    shifted = [pltpu.roll(x, 1, 1) * behind, x, pltpu.roll(x, frame_dev - 1, 1) * ahead]
    taps = [pltpu.roll(v, (1 - i) % rows, 0) if i != 1 else v for i in range(3) for v in shifted]
    features = feature_rows(centre, (taps, inner))
    lane = iota((1, 128), 1)
    features = jnp.where(lane == 90, centre, jnp.where(lane == 91, number, features))
    pick = iota((8, frame_dev), 0)
    column = jnp.where(pick < 4, pick, frame_dev - 8 + pick)
    strip = dot((iota((8, frame_dev), 1) == column).astype(BF16), x.astype(BF16), ((1,), (1,)))
    lane = iota((8, 128), 1)
    repeat = (iota((rows, 128), 1) % rows == iota((rows, 128), 0)).astype(BF16)
    strip = jnp.where(lane // rows == iota((8, 128), 0), dot(strip.astype(BF16), repeat), 0.0)
    strip = jnp.sum(strip, axis=0, keepdims=True)

    def put(n, value):
        rows_out[pl.ds(n, devices, stride=FIRST), :] = jnp.broadcast_to(value, (devices, 128))

    near = jnp.concatenate([x[0:2], x[rows - 2 :]], axis=0)
    near = jnp.concatenate([near[:, :128], near[:, 128:]], axis=0)
    for d in range(devices):
        rows_out[FIRST * d : FIRST * d + 8, :] = near
    put(COLUMNS, strip)
    copies[2].wait()
    _, chan, many, half = own.shape
    share = share_of(devices, chan)
    holders = chan // share
    g = own[0].astype(F32)
    edges[0:chan] = g[:, 0, :]
    edges[chan:] = g[:, many - 1, :]

    def spread_out(v, held):
        if held < devices:
            v = jnp.concatenate([v, jnp.zeros((devices - held, 128), F32)], axis=0)
        return v

    for n in range(share):
        put(EDGES + n, spread_out(edges[n * holders : (n + 1) * holders, :], holders))
        put(EDGES + share + n, spread_out(edges[chan + n * holders : chan + (n + 1) * holders, :], holders))
    for n in range(2 * share, COLUMNS - EDGES):
        put(EDGES + n, jnp.zeros((1, 128), F32))
    end = iota((8, half), 0)
    at = iota((8, half), 1)
    ends = ((end == 0) & (at == 0)) | ((end == 1) & (at == half - 1))
    columns = dot(ends.astype(BF16), g.reshape(chan * many, half).astype(BF16), ((1,), (1,)))
    group = 128 // many
    source = iota((128, 128), 0)
    lane = iota((group, 128), 1)
    mine = lane // many == iota((group, 128), 0)
    lane8, own8 = iota((8, 128), 1), iota((8, 128), 0)
    parts = three_parts(features)
    for n in range(2):
        side = jnp.zeros((holders, 128), F32)
        for m in range(share):
            move = (iota((128, 128), 1) == SIDE + many * m + source % many).astype(BF16)
            first = m * holders * many // 128
            block = [columns[n : n + 1, 128 * q : 128 * (q + 1)] for q in range(first, first + holders * many // 128)]
            block = jnp.concatenate([jnp.where(mine, v, 0.0) for v in block], axis=0)
            side = side + dot(block.astype(BF16), move)
        far = x[2:4] if n == 0 else x[rows - 4 : rows - 2]
        pieces = [far[r : r + 1, 128 * h : 128 * (h + 1)] for r in range(2) for h in range(2)]
        pieces = jnp.concatenate([jnp.where(lane8 // 16 == own8, v, 0.0) for v in pieces], axis=0)
        far = dot(pieces.astype(BF16), (iota((128, 128), 1) == FAR + source % 16).astype(BF16))
        put(SUMS + n, spread_out(side, holders) + spread_out(far, FAR_HOLDERS) + parts[n])
    put(SUMS + 2, parts[2])
    out[...] = rows_out[...].reshape(out.shape).astype(BF16)


def weights(own, bounds_hbm, k2_hbm, k1_hbm, gain_one_hbm, bias_one_hbm, gain_two_hbm, bias_two_hbm,
            wf, wb, w1, ws_hbm, pairs, singles, k1t, params, all_masks, edge_masks, twice, own_rows,
            k2, k1, vectors, bounds, ws, temp, sems):
    loads = start_all(
        (bounds_hbm, bounds),
        (k2_hbm, k2),
        (k1_hbm, k1),
        (gain_one_hbm, vectors.at[0]),
        (bias_one_hbm, vectors.at[1]),
        (gain_two_hbm, vectors.at[2]),
        (bias_two_hbm, vectors.at[3]),
        sems=sems,
    )
    _, many, count, half = own.shape
    temp[...] = own[0].astype(F32).reshape(many * count, half)
    for r in range(count):
        own_rows[r * many : (r + 1) * many] = temp[pl.ds(r, many, stride=count), :].astype(BF16)
    wait_all(loads)
    chan = k2.shape[1]
    span = wf.shape[1]
    taps = [k2[t].astype(F32) for t in range(9)]
    rest = jnp.zeros((chan, span - 9 * chan), F32)
    forward = jnp.concatenate(taps + [rest], axis=1)
    backward = jnp.concatenate([taps[8 - t].T for t in range(9)] + [rest], axis=1)
    for r in range(wb.shape[0] // chan):
        at = slice(r * chan, (r + 1) * chan)
        wb[at] = (pltpu.roll(backward, 3 * chan * r, 1) if r else backward).astype(BF16)
    full = jnp.concatenate([k1[n].astype(F32) for n in range(3)] + [jnp.zeros((7, chan), F32)], axis=0)
    low = [
        jnp.concatenate([full[3 * (2 - a) + 2 - b : 3 * (2 - a) + 3 - b] for a in range(3)], axis=1)
        for b in range(3)
    ]
    rest = jnp.zeros((1, ws.shape[1] - 3 * chan), F32)
    for b in range(3):
        base = jnp.concatenate([low[b], rest], axis=1)
        many = ws.shape[0] // 3
        rolled = [pltpu.roll(base, chan * m, 1) if m else base for m in range(many)]
        ws[many * b : many * (b + 1)] = jnp.concatenate(rolled, axis=0).astype(BF16)
    store_ws = pltpu.make_async_copy(ws, ws_hbm, sems.at[7])
    store_ws.start()
    count, frame_dev = all_masks.shape[0] // 3, all_masks.shape[1]
    frames = iota((count, frame_dev), 0) * frame_dev + iota((count, frame_dev), 1)
    for n, mask in enumerate(frame_masks(bounds[...], frames)):
        all_masks[n * count : (n + 1) * count] = mask
    q = iota(edge_masks.shape, 0)
    lane = iota(edge_masks.shape, 1)
    k = q % 8
    frames = (q // 8) * frame_dev + jnp.where(k < 4, k, k + frame_dev - 8)
    living, behind, ahead = frame_masks(bounds[...], frames)
    living = jnp.where((k == 0) | (k == 7), living, 0.0)
    edge_masks[...] = jnp.where(lane == 0, living, jnp.where(lane == 1, behind, jnp.where(lane == 2, ahead, 0.0)))
    params[...] = jnp.concatenate(
        [vectors[n] for n in range(4)] + [jnp.zeros((4, chan), F32)], axis=0
    )
    tap = iota((16, 128), 0)
    lane = iota((16, 128), 1)
    i = (tap * 11) >> 5
    ninth = (lane * 57) >> 9
    to_band = (lane == BAND * (tap - 3 * i) + i) & (tap < 9)
    to_left = (ninth == tap) & (tap < 9)
    to_right = (lane - 9 * ninth == tap) & (lane < 81)
    to_single = (lane == 81 + tap) & (tap < 9)
    source = iota((128, 128), 0) - 81
    lane = iota((128, 128), 1)
    ninth = (lane * 57) >> 9
    inside = (source >= 0) & (source < 9) & (lane < 81)
    twice[...] = jnp.where(inside, (source == ninth).astype(F32) + (source == lane - 9 * ninth).astype(F32), 0.0)
    for r in range(wf.shape[0] // chan):
        at = slice(r * chan, (r + 1) * chan)
        wf[at] = (pltpu.roll(forward, 3 * chan * r, 1) if r else forward).astype(BF16)
    k1t[...] = full
    k = full.astype(BF16)
    lanes = [dot(k, select.astype(BF16), ((0,), (0,))) for select in (to_band, to_left, to_right, to_single)]
    pairs[...] = lanes[1] * lanes[2]
    singles[...] = lanes[3]
    for m in range(w1.shape[0] // chan):
        w1[m * chan : (m + 1) * chan] = (pltpu.roll(lanes[0], m, 1) if m else lanes[0]).astype(BF16)
    store_ws.wait()


def feature_rows(centre, *parts):
    def folded(v):
        return jnp.sum(halves(v), axis=0, keepdims=True)

    rows = [jnp.zeros((1, 128), F32)] * 96
    for taps, weight in parts:
        z = [tap - centre for tap in taps]
        for s in range(9):
            left = z[s] * weight
            rows[81 + s] = rows[81 + s] + folded(left)
            for t in range(s, 9):
                rows[9 * s + t] = rows[9 * t + s] = rows[9 * s + t] + folded(left * z[t])
    return to_lanes(jnp.sum(jnp.concatenate(rows, axis=0), axis=1, keepdims=True))


def summed_blocks(ref, devices, by=1):
    block = ref.shape[0] // devices
    period = max(8 // math.gcd(block, 8), by)
    step = period * block
    total = ref[0:step, :]
    for at in range(step, ref.shape[0], step):
        total = total + ref[at : at + step, :]
    results = []
    for first in range(by):
        result = total[first * block : (first + 1) * block]
        for n in range(first + by, period, by):
            result = result + total[n * block : (n + 1) * block]
        results.append(result)
    return results if by > 1 else results[0]


def moved_rows(v, step):
    if step == 0:
        return v
    count = v.shape[0]
    if abs(step) >= count:
        return jnp.zeros_like(v)
    zero = jnp.zeros((abs(step), v.shape[1]), v.dtype)
    if step > 0:
        return jnp.concatenate([zero, v[: count - step]], axis=0)
    return jnp.concatenate([v[-step:], zero], axis=0)


def silu_halves(h):
    t = jnp.tanh(h)
    one = 1.0 + t
    return h * one, one * (1.0 + h * (1.0 - t))


def act_row(act, r, low, low_masks):
    low = low * low_masks[0]
    chan = low.shape[0]
    for n, v in enumerate((low,) + shifted_frames(low, *low_masks[1:])):
        at = (3 * r + (1, 0, 2)[n]) * chan
        act[at : at + chan, :] = v


def forward_one(recv, spec, pairs, singles, twice, w1, wf, params, masks, all_masks, edge_masks,
                pre_two, payload, act, x3, far_rim, stats, features_out, pre_one, got, strips, halo, rows_out):
    devices = recv.shape[0]
    n_mel, count = lax.axis_size("mel"), lax.axis_size("tm")
    rows = MEL_ROWS
    mels = n_mel * rows
    wide = masks.shape[1]
    frame_dev = wide - RIM
    chan = params.shape[1]
    me_m, me_t = lax.axis_index("mel"), lax.axis_index("tm")
    usable, behind, ahead = (masks[n : n + 1] for n in range(3))
    total = masks[3:4, 0:1]
    got[...] = recv[...].astype(F32).reshape(devices * FIRST, 128)

    def every(n):
        return got[pl.ds(n, devices, stride=FIRST), :]

    lane = iota((count, 128), 1)
    bands = [got[pl.ds(FIRST * k * count + COLUMNS, count, stride=FIRST), :] for k in range(n_mel)]
    for c in range(8):
        column = jnp.zeros((count, 128), F32)
        for k, band in enumerate(bands):
            part = jnp.where(lane // rows == c, band, 0.0)
            column = column + (pltpu.roll(part, rows * (k - c) % 128, 1) if k != c else part)
        strips[pl.ds(c, count, stride=8), :] = column
    at = pl.multiple_of(FIRST * (jnp.maximum(me_m - 1, 0) * count + me_t), 8)
    above = got[pl.ds(at, 8), :] * (me_m > 0).astype(F32)
    at = pl.multiple_of(FIRST * (jnp.minimum(me_m + 1, n_mel - 1) * count + me_t), 8)
    below = got[pl.ds(at, 8), :] * (me_m < n_mel - 1).astype(F32)
    above = jnp.concatenate([above[2:4], above[6:8]], axis=1)
    below = jnp.concatenate([below[0:2], below[4:6]], axis=1)
    own = spec[0].astype(F32) * usable[:, :frame_dev]
    at = pl.multiple_of(8 * jnp.minimum(me_t + 1, count - 1), 8)
    after = strips[pl.ds(at, 8), :][:, :mels] * (me_t + 1 < count).astype(F32)
    at = pl.multiple_of(8 * jnp.maximum(me_t - 1, 0), 8)
    before = strips[pl.ds(at, 8), :][:, :mels] * (me_t > 0).astype(F32)
    sides = jnp.concatenate([after[0:4], before[4:8], jnp.zeros((8, mels), F32)], axis=0).astype(BF16)
    side = iota((16, RIM), 0)
    place = iota((16, RIM), 1) == jnp.where(side < 4, side, jnp.where(side < 8, side + RIM - 8, -1))
    halo[0:8] = jnp.zeros((8, RIM), F32)
    halo[mels : mels + 8] = jnp.zeros((8, RIM), F32)
    halo[4 : mels + 4] = dot(sides, place.astype(BF16), ((0,), (0,)))
    rim = halo[pl.ds(pl.multiple_of(me_m * rows, 8), BAND), :]
    far_rim[...] = rim
    row = iota((BAND, RIM), 0)
    rim = jnp.where((row >= 2) & (row < BAND - 2), rim, 0.0)
    blank = jnp.zeros((2, frame_dev), F32)
    near = jnp.concatenate([jnp.concatenate([blank, above, own, below, blank], axis=0), rim], axis=1)
    x3[...] = jnp.concatenate(
        [
            pltpu.roll(near, 1, 1) * behind,
            near,
            pltpu.roll(near, wide - 1, 1) * ahead,
            jnp.broadcast_to(usable, (BAND, wide)),
            jnp.zeros((128 - 4 * BAND, wide), F32),
        ],
        axis=0,
    ).astype(BF16)
    pre_one[2 * chan : (rows + 4) * chan] = dot(w1[2 * chan : (rows + 4) * chan, :], x3[...])
    lane = iota((1, 128), 1)
    parts = jnp.where(lane < 92, every(SUMS) + every(SUMS + 1) + every(SUMS + 2), 0.0)
    centres, numbers = parts[:, 90:91], parts[:, 91:92]
    centre = jnp.sum(centres * numbers, axis=0, keepdims=True)
    centre = centre / jnp.maximum(jnp.sum(numbers, axis=0, keepdims=True), 1.0)
    delta = centres - centre
    features = jnp.sum(parts + delta * numbers * jnp.where(lane < 81, delta, 1.0), axis=0, keepdims=True)
    moved = jnp.sum(delta * parts, axis=0, keepdims=True)
    def edge_row(k, n):
        first = FIRST * k * count + n
        return jnp.concatenate(
            [got[pl.ds(first, count, stride=FIRST), :], got[pl.ds(first + 4, count, stride=FIRST), :]], axis=1
        )

    edge_rows = [[edge_row(k, n) for n in range(4)] for k in range(n_mel)]
    zero = jnp.zeros((count, frame_dev), F32)
    rows_of = [[], [], []]
    for k, (top, second, fore, bottom) in enumerate(edge_rows):
        for n, v in enumerate((edge_rows[k - 1][3] if k else zero, top, second)):
            rows_of[n].append(v)
        for n, v in enumerate((fore, bottom, edge_rows[k + 1][0] if k + 1 < n_mel else zero)):
            rows_of[n].append(v)
    f_usable, f_behind, f_ahead = (all_masks[n * count : (n + 1) * count, :] for n in range(3))
    lane = iota((count, frame_dev), 1)

    def frame_before(v):
        v = pltpu.roll(v, 1, 1)
        return jnp.where(lane == 0, pltpu.roll(v, 1, 0), v) * f_behind

    def frame_after(v):
        v = pltpu.roll(v, frame_dev - 1, 1)
        return jnp.where(lane == frame_dev - 1, pltpu.roll(v, count - 1, 0), v) * f_ahead

    taps = []
    for group in rows_of:
        for move in (frame_before, lambda v: v, frame_after):
            taps.append(jnp.concatenate([move(v) for v in group], axis=1))
    f_usable = jnp.concatenate([f_usable] * (2 * n_mel), axis=1)
    borders = (taps, f_usable)
    edge = strips[...]
    q_usable, q_behind, q_ahead = (edge_masks[:, n : n + 1] for n in range(3))
    lane = iota((count * 8, 128), 1)
    inside = (lane < mels) & (lane % rows != 0) & (lane % rows != rows - 1)
    shifted = [
        pltpu.roll(edge, 1, 0) * q_behind,
        edge,
        pltpu.roll(edge, count * 8 - 1, 0) * q_ahead,
    ]
    taps = [pltpu.roll(v, (1 - i) % 128, 1) if i != 1 else v for i in range(3) for v in shifted]
    features = features + feature_rows(centre, borders, (taps, jnp.where(inside, q_usable, 0.0)))
    features = jnp.where(iota((1, 128), 1) < 90, features, 0.0)
    near_mean = jnp.sum(singles[...] * features, axis=1, keepdims=True) / total
    around = jnp.sum(singles[...], axis=1, keepdims=True)
    square = jnp.sum(pairs[...] * features, axis=1, keepdims=True)
    square = (square + 2.0 * around * jnp.sum(singles[...] * moved, axis=1, keepdims=True)) / total
    inv = lax.rsqrt(square - near_mean * near_mean + 1e-05)
    mean = near_mean + centre * around
    lane = iota((chan, 128), 1)
    stats[0:chan] = jnp.where(lane == 0, mean, jnp.where(lane == 1, inv, 0.0))
    stats[chan : chan + 8] = jnp.broadcast_to(to_lanes(near_mean), (8, 128))
    stats[chan + 8 : chan + 16] = jnp.broadcast_to(to_lanes(inv), (8, 128))
    scale = 0.5 * to_column(params[0:1], chan) * inv
    shift = 0.5 * to_column(params[1:2], chan) - mean * scale
    stats[chan + 16 :] = jnp.where(lane == 0, scale, jnp.where(lane == 1, shift, 0.0))
    scale = jnp.broadcast_to(scale, (chan, wide))
    shift = jnp.broadcast_to(shift, (chan, wide))
    block, taps = wf.shape
    first = jnp.zeros((chan, 128), F32)
    second = jnp.zeros((chan, 128), F32)
    own_mask = usable[:, :frame_dev]
    low_masks = [m.astype(BF16) for m in (usable, behind, ahead)]
    for r in range(2, rows + 4):
        value, _ = silu_halves(pre_one[r * chan : (r + 1) * chan, :] * scale + shift)
        if not 0 <= r - 3 < rows:
            value = value * row_valid(r - 3, rows)
        act_row(act, r, value.astype(BF16), low_masks)
        if r < 5 or r % 2 == 0:
            continue
        g = (r - 3) // 2
        result = dot(wf[...], act[g * 3 * block : g * 3 * block + taps, :frame_dev])
        at = (g - 1) * block
        pre_two[at : at + block, :frame_dev] = result
        if g % 2 == 0:
            beside = [act[n * 3 * block : n * 3 * block + taps, frame_dev:] for n in (g - 1, g)]
            beside = dot(wf[...], jnp.concatenate(beside, axis=1))
            for n in range(2):
                pre_two[at + (n - 1) * block : at + n * block, frame_dev:] = beside[:, n * RIM : (n + 1) * RIM]
        for q in range(2):
            p = result[q * chan : (q + 1) * chan]
            masked = p * own_mask
            first = first + halves(masked)
            second = second + halves(masked * p)
    moved = dot(jnp.broadcast_to(moved, (8, 128)), twice[...], precision=EXACT)[0:1]
    features_out[...] = jnp.concatenate(
        [features + moved, jnp.broadcast_to(centre, (1, 128)), jnp.zeros((6, 128), F32)], axis=0
    )
    share = share_of(devices, chan)

    def put(n, value):
        rows_out[pl.ds(n, devices, stride=SECOND), :] = jnp.broadcast_to(value, (devices, 128))

    for n in range(share):
        put(3 + n, moved_rows(every(EDGES + share + n), count))
        put(3 + share + n, moved_rows(every(EDGES + n), -count))
    for n in [0, 1, 2] + list(range(3 + 2 * share, SECOND - 1)):
        put(n, jnp.zeros((1, 128), F32))
    lane = iota((devices, 128), 1)
    tm = iota((devices, 128), 0) % count
    at_side = (lane >= SIDE) & (lane < FAR)
    lefts = jnp.where(at_side, every(SUMS), 0.0)
    rights = jnp.where(at_side, every(SUMS + 1), 0.0)
    beside = jnp.zeros((devices, 128), F32)
    for n, step in enumerate((0, count, -count)):
        one = jnp.where(tm > 0, moved_rows(rights, step + 1), 0.0)
        two = jnp.where(tm < count - 1, moved_rows(lefts, step - 1), 0.0)
        beside = beside + pltpu.roll(one, (32 * n - SIDE) % 128, 1) + pltpu.roll(two, (32 * n + 16 - SIDE) % 128, 1)
    outer = jnp.where(lane >= FAR, moved_rows(every(SUMS + 1), count), 0.0)
    beside = beside + pltpu.roll(outer, 128 - 16, 1)
    beside = beside + jnp.where(lane >= FAR, moved_rows(every(SUMS), -count), 0.0)
    put(SECOND - 1, beside)
    first = jnp.sum(first, axis=1, keepdims=True)
    second = jnp.sum(second, axis=1, keepdims=True)
    parts = list(three_parts(to_lanes(first) + to_lanes(second, chan)))
    parts = jnp.concatenate(parts + [jnp.zeros((SECOND - 3, 128), F32)], axis=0)
    for d in range(devices):
        payload[d] = (rows_out[SECOND * d : SECOND * (d + 1), :] + parts).astype(BF16)


def spreading(half):
    lane = iota((half, 2 * half), 1)
    return jnp.where(lane >> 1 == iota((half, 2 * half), 0), 0.25, 0.0).astype(BF16)


def half_share(devices, taps):
    return -(-taps // 2 // devices)


def backward_scaled(recv, pre_two, act, own_rows, params, masks,
                    grad, kept_half, sent_half, totals, stats, pairs, up, right, halved):
    devices = recv.shape[0]
    chan = params.shape[1]
    half = own_rows.shape[1]
    frame_dev = 2 * half
    rows = MEL_ROWS
    up[...] = dot(own_rows[...], spreading(half))
    usable = masks[0:1, :frame_dev]
    total = masks[3:4, 0:1]
    sums = [recv[d].astype(F32) for d in range(devices)]
    while len(sums) > 1:
        sums = [a + b for a, b in zip(sums[0::2], sums[1::2])]
    sums = jnp.sum(sums[0][0:3], axis=0, keepdims=True)
    mean = to_column(sums, chan) / total
    inv = lax.rsqrt(to_column(sums, chan, chan) / total - mean * mean + 1e-05)
    scale = 0.5 * to_column(params[2:3], chan) * inv
    shift = 0.5 * to_column(params[3:4], chan) - mean * scale
    lane = iota((chan, 128), 1)
    columns = jnp.zeros((chan, 128), F32)
    for n, column in enumerate((mean, inv, scale, shift)):
        columns = jnp.where(lane == n, column, columns)
    stats[0:chan] = columns
    stats[chan : chan + 8] = jnp.broadcast_to(to_lanes(inv), (8, 128))
    mean, inv, scale, shift = (jnp.broadcast_to(v, (chan, frame_dev)) for v in (mean, inv, scale, shift))
    first = jnp.zeros((chan, 128), F32)
    second = jnp.zeros((chan, 128), F32)
    mask = 0.5 * usable
    right[3 * chan :] = jnp.ones((16, rows * frame_dev), BF16)
    table = jnp.zeros((9 * chan, 3 * chan + 16), F32)
    for m in range(rows):
        at = slice(m * chan, (m + 1) * chan)
        pre = pre_two[at, :frame_dev]
        value, slope = silu_halves(pre * scale + shift)
        value = value * usable
        both = value if m % 2 == 0 else both + value
        if m % 2:
            pairs[m // 2 * chan : (m // 2 + 1) * chan, :] = both
        g = up[m // 2 * chan : (m // 2 + 1) * chan, :] * slope * mask
        grad[at, :] = g
        normed = (pre - mean) * inv
        first = first + halves(g * normed)
        second = second + halves(g)
        lanes = slice(m * frame_dev, (m + 1) * frame_dev)
        right[0:chan, lanes] = g.astype(BF16)
        right[chan : 2 * chan, lanes] = normed.astype(BF16)
        right[2 * chan : 3 * chan, lanes] = (g - right[0:chan, lanes].astype(F32)).astype(BF16)
        if m % 8 == 7:
            start = m - 7
            left = [act[(n + 2) * 3 * chan : (n + 5) * 3 * chan, :frame_dev] for n in range(start, m + 1)]
            lanes = slice(start * frame_dev, (m + 1) * frame_dev)
            table = table + dot(jnp.concatenate(left, axis=1), right[:, lanes], ((1,), (1,)))
    first = jnp.sum(first, axis=1, keepdims=True)
    second = jnp.sum(second, axis=1, keepdims=True)
    totals[...] = jnp.broadcast_to(to_lanes(first) + to_lanes(second, chan), (8, 128))
    rest = jnp.concatenate([table[:, 2 * chan :], jnp.zeros((9 * chan, chan - 16), F32)], axis=1)
    both = table[:, : 2 * chan] + jnp.where(iota(rest.shape, 1) < chan, rest, 0.0)
    single = rest[:, chan : chan + 1]
    taps = 9 * chan // 2
    lane = iota((devices, 128), 1)
    for h in range(2):
        halved[h, 0:taps] = both[h * taps : (h + 1) * taps]
        constants = jnp.zeros((devices, 128), F32)
        for k in range(half_share(devices, 9 * chan)):
            at = h * taps + k * devices
            ones = single[at : min(at + devices, (h + 1) * taps)]
            if ones.shape[0] < devices:
                ones = jnp.concatenate([ones, jnp.zeros((devices - ones.shape[0], 1), F32)], axis=0)
            constants = jnp.where(lane == k, ones, constants)
        halved[h, taps:] = constants
    core = lax.axis_index("tm") % 2
    kept_half[...] = halved[core]
    sent_half[...] = halved[1 - core]


def around(recv, pre_two, act, w1, wf, x3, far_rim, stats_one, masks, stats, pre_ring, ring, rim,
           sides, up, got, beyond, more):
    devices = recv.shape[0]
    got[...] = recv[:, 0:SECOND, :].astype(F32).reshape(devices * SECOND, 128)
    rows = MEL_ROWS
    many = rows // 2
    wide = pre_two.shape[1]
    frame_dev = wide - RIM
    chan = pre_two.shape[0] // rows
    usable = masks[0:1]
    low_masks = [masks[n : n + 1].astype(BF16) for n in range(3)]
    pieces = got[pl.ds(SECOND - 1, devices, stride=SECOND), :][:FAR_HOLDERS].astype(BF16)
    source = iota((128, 128), 0)
    lane = iota((FAR_HOLDERS, 128), 1)
    mine = lane // 16 == iota((FAR_HOLDERS, 128), 0) % 8
    outer = []
    for first in (SIDE, FAR):
        place = (source - first == iota((128, 128), 1) % 16).astype(BF16)
        v = jnp.where(mine, dot(pieces, place), 0.0)
        v = [jnp.sum(v[8 * n : 8 * n + 8], axis=0, keepdims=True) for n in range(4)]
        outer += [jnp.concatenate(v[2 * r : 2 * r + 2], axis=1) for r in range(2)]
    blank = jnp.zeros((BAND - 4, frame_dev), F32)
    far = jnp.concatenate(outer[:2] + [blank] + outer[2:], axis=0)
    row = iota((BAND, RIM), 0)
    far = jnp.concatenate([far, jnp.where((row < 2) | (row >= BAND - 2), far_rim[...], 0.0)], axis=1)
    far = jnp.concatenate(
        [
            pltpu.roll(far, 1, 1) * masks[1:2],
            far,
            pltpu.roll(far, wide - 1, 1) * masks[2:3],
            jnp.zeros((128 - 3 * BAND, wide), F32),
        ],
        axis=0,
    )
    x_all = (x3[...].astype(F32) + far).astype(BF16)
    scale = jnp.broadcast_to(stats_one[chan + 16 :, 0:1], (chan, wide))
    shift = jnp.broadcast_to(stats_one[chan + 16 :, 1:2], (chan, wide))
    for h, start in enumerate((0, rows + 4)):
        pre_one = dot(w1[start * chan : (start + 2) * chan, :], x_all)
        for n in range(2):
            value, _ = silu_halves(pre_one[n * chan : (n + 1) * chan] * scale + shift)
            value = value * row_valid(start + n - 3, rows)
            act_row(more, 2 * h + n, value.astype(BF16), low_masks)
    line = 3 * chan
    above = jnp.concatenate([more[0 : 2 * line, :], act[2 * line : 4 * line, :]], axis=0)
    below = jnp.concatenate([act[(rows + 2) * line : (rows + 4) * line, :], more[2 * line :, :]], axis=0)
    pre_ring[0 : 2 * chan] = dot(wf[...], above)
    pre_ring[2 * chan :] = dot(wf[...], below)
    share = share_of(devices, chan)
    holders = chan // share

    def every(n):
        return got[pl.ds(n, devices, stride=SECOND), :]

    beside = 0.25 * every(SECOND - 1)[:holders]
    lane = iota((holders, RIM), 1)
    for n in range(share):
        first = n * holders
        beyond[first : first + holders, :] = every(3 + n)[:holders]
        beyond[chan + first : chan + first + holders, :] = every(3 + share + n)[:holders]
        for r in range(many + 2):
            at = many * n + (r if r < many else 32 + many - 1 if r == many else 64)
            left, right_of = beside[:, at : at + 1], beside[:, at + 16 : at + 17]
            side = jnp.where(lane >= RIM - 2, left, jnp.where(lane < 2, right_of, 0.0))
            sides[r * chan + first : r * chan + first + holders, :] = side
    up[...] = dot(beyond[...].astype(BF16), spreading(frame_dev // 2))
    scale = jnp.broadcast_to(stats[0:chan, 2:3], (chan, wide))
    shift = jnp.broadcast_to(stats[0:chan, 3:4], (chan, wide))
    for n, m in enumerate((-2, -1, rows, rows + 1)):
        below = n // 2
        upstream = jnp.concatenate(
            [
                up[below * chan : (below + 1) * chan, :],
                sides[(many + below) * chan : (many + below + 1) * chan, :],
            ],
            axis=1,
        )
        _, slope = silu_halves(pre_ring[n * chan : (n + 1) * chan, :] * scale + shift)
        ring[n * chan : (n + 1) * chan, :] = upstream * slope * (usable * (0.5 * row_valid(m, rows)))
    for m in range(rows):
        at = slice(m * chan, (m + 1) * chan)
        _, slope = silu_halves(pre_two[at, frame_dev:] * scale[:, frame_dev:] + shift[:, frame_dev:])
        upstream = sides[m // 2 * chan : (m // 2 + 1) * chan, :]
        rim[m * chan : (m + 1) * chan, :] = upstream * slope * (0.5 * usable[:, frame_dev:])


def pack_sums(kept_half, received, totals, after, payload):
    del after
    devices = kept_half.shape[0] - TAPS // 2
    block = payload.shape[0] // devices
    payload[pl.ds(0, devices, stride=block), :] = jnp.broadcast_to(totals[0:1], (devices, 128))
    taps = TAPS // 2
    total = kept_half[...] + received[...]
    for k in range(block - 2):
        cut = total[k * devices : min((k + 1) * devices, taps)]
        if cut.shape[0] < devices:
            cut = jnp.concatenate([cut, jnp.zeros((devices - cut.shape[0], 128), F32)], axis=0)
        payload[pl.ds(1 + k, devices, stride=block), :] = cut
    payload[pl.ds(block - 1, devices, stride=block), :] = total[taps:]


def pool(totals, pairs, out, gain_out, bias_out, temp):
    gain_out[...] = totals[0:1, : gain_out.shape[1]]
    bias_out[...] = totals[0:1, gain_out.shape[1] :]
    chan, rows, half = out.shape[1:]
    to_mean = jnp.where(iota((2 * half, half), 0) >> 1 == iota((2 * half, half), 1), 0.25, 0.0)
    pooled = dot(pairs[...], to_mean, precision=EXACT)
    for r in range(rows):
        temp[pl.ds(r, chan, stride=rows), :] = pooled[r * chan : (r + 1) * chan]
    out[0] = temp[...].reshape(chan, rows, half).astype(BF16)


def backward(recv, pre_two, pre_ring, grad, ring, rim, stats_two, w1, x3, stats, params, masks, wb,
             out, own_low, payload, totals, g3, pre_one, g1):
    chan = params.shape[1]
    rows = MEL_ROWS
    wide = pre_two.shape[1]
    frame_dev = wide - RIM
    usable = masks[0:1]
    behind, ahead = (masks[n : n + 1].astype(BF16) for n in (1, 2))
    total = masks[3:4, 0:1]
    devices = payload.shape[0]
    pre_one[...] = dot(w1[3 * chan : (rows + 3) * chan], x3[:, :frame_dev])

    even, odd = summed_blocks(recv, devices, 2)
    sums = even[0:1] + odd[0:1]
    gain_sum, bias_sum = sums[:, :chan], sums[:, chan:]
    totals[...] = jnp.broadcast_to(sums, (8, 128))
    mean, inv = stats_two[0:chan, 0:1], stats_two[0:chan, 1:2]
    factor = to_column(params[2:3], chan) * inv
    gain_part = factor * (to_column(sums, chan) / total * inv)
    bias_part = factor * (to_column(sums, chan, chan) / total) - mean * gain_part
    gain_part = jnp.broadcast_to(gain_part, (chan, wide))
    bias_part = jnp.broadcast_to(bias_part, (chan, wide))
    factor = jnp.broadcast_to(factor, (chan, wide))
    scale = jnp.broadcast_to(stats[chan + 16 :, 0:1], (chan, frame_dev))
    shift = jnp.broadcast_to(stats[chan + 16 :, 1:2], (chan, frame_dev))
    factor_one = jnp.broadcast_to(to_column(params[0:1], chan) * stats[0:chan, 1:2], (chan, frame_dev))
    own_mask = 0.5 * usable[:, :frame_dev]
    count = rows + 4
    share = even.shape[0] - 2
    mine = jnp.concatenate([even[1 : share + 1], odd[1 : share + 1]], axis=0)
    single = jnp.concatenate([to_column(v[share + 1 :], share) for v in (even, odd)], axis=0)
    factor_l = params[2:3] * stats_two[chan : chan + 1, :chan]
    mine = mine[:, :chan] - (bias_sum * single + gain_sum * mine[:, chan:]) / total
    mine = factor_l * mine
    mine = jnp.concatenate([mine[:share], mine[share:]], axis=1)
    if share < 9:
        mine = jnp.concatenate([mine, jnp.zeros((9 - share, 128), F32)], axis=0)
    table = jnp.zeros((chan, 128), F32)

    def tap_sums(m):
        taps_in = jnp.concatenate([x3[:, :frame_dev]] * 2, axis=1)
        products = dot(g1[m * chan : (m + 4) * chan, :], taps_in, ((1,), (1,)))
        moved = [pltpu.roll(products[k * chan : (k + 1) * chan], 128 - (m + k + 3), 1) for k in range(4)]
        return (moved[0] + moved[1]) + (moved[2] + moved[3])

    for q in range(count):
        at = slice(q * chan, (q + 1) * chan)
        mask = usable if 0 <= q - 2 < rows else usable * row_valid(q - 2, rows)
        if 2 <= q < rows + 2:
            own = slice((q - 2) * chan, (q - 1) * chan)
            pre, scaled = pre_two[own, :], jnp.concatenate([grad[own, :], rim[own, :]], axis=1)
        else:
            n = q if q < 2 else q - rows
            pre, scaled = pre_ring[n * chan : (n + 1) * chan, :], ring[n * chan : (n + 1) * chan, :]
        low = (factor * scaled - (bias_part + pre * gain_part) * mask).astype(BF16)
        out[at, :] = low
        if not 1 <= q < count - 1:
            continue
        base = (q - 1) * 3 * chan
        for n, v in enumerate((low,) + shifted_frames(low, behind, ahead)):
            spot = base + (1, 0, 2)[n] * chan
            g3[spot : spot + chan, :] = v[:, :frame_dev]
        start = q - 4
        if start < 0 or start % 2:
            continue
        result = dot(wb[...], g3[start * 3 * chan : (start + 4) * 3 * chan, :])
        for n in range(2):
            m = start + n
            at = slice(m * chan, (m + 1) * chan)
            _, slope = silu_halves(pre_one[at, :] * scale + shift)
            value = result[n * chan : (n + 1) * chan] * slope * own_mask
            own_low[at, :] = (value * factor_one).astype(BF16)
            g1[at, :frame_dev] = value.astype(BF16)
            g1[at, frame_dev:] = (value - g1[at, :frame_dev].astype(F32)).astype(BF16)
        if start % 4 == 2 and start > 2:
            table = table + tap_sums(start - 6)
    table = table + tap_sums(rows - 4)
    table = table.T
    places = [BAND * j + i for i in range(3) for j in range(3)] + [3 * BAND]
    rows10 = jnp.concatenate([table[n : n + 1] for n in places], axis=0)
    sums = jnp.concatenate([rows10[0:5], rows10[5:10]], axis=1)
    block = jnp.concatenate(list(three_parts(sums)) + [mine], axis=0).astype(BF16)
    for d in range(devices):
        payload[d] = block


def transposed(grad, own_low, w1, wb, x3, stats, features, k1t, params, masks, ws_hbm,
               first, ws, normed_taps, low, g3, rim, sem):
    load = pltpu.make_async_copy(ws_hbm, ws, sem)
    load.start()
    rows = MEL_ROWS
    chan = own_low.shape[0] // rows
    wide = grad.shape[1]
    frame_dev = wide - RIM
    count = grad.shape[0] // chan
    usable = masks[0:1]
    behind, ahead = (masks[n : n + 1].astype(BF16) for n in (1, 2))
    scale = jnp.broadcast_to(stats[chan + 16 :, 0:1], (chan, wide))
    shift = jnp.broadcast_to(stats[chan + 16 :, 1:2], (chan, wide))
    factor = jnp.broadcast_to(to_column(params[0:1], chan) * stats[0:chan, 1:2], (chan, wide))
    edge = (0, 1, 2, 3, count - 4, count - 3, count - 2, count - 1)
    for q in range(count):
        value = grad[q * chan : (q + 1) * chan, :]
        for n, v in enumerate((value,) + shifted_frames(value, behind, ahead)):
            spot = (3 * q + (1, 0, 2)[n]) * chan
            rim[spot : spot + chan, :] = v[:, frame_dev:]
            if q in edge:
                spot = (3 * edge.index(q) + (1, 0, 2)[n]) * chan
                g3[spot : spot + chan, :] = v[:, :frame_dev]
    low[chan : (rows + 1) * chan, :frame_dev] = own_low[...]

    def put(m, lanes, result, pre_one):
        at = slice((m + 1) * chan, (m + 2) * chan)
        _, slope = silu_halves(pre_one * scale[:, lanes] + shift[:, lanes])
        mask = usable[:, lanes] * (0.5 * row_valid(m, rows))
        low[at, lanes] = (result * slope * mask * factor[:, lanes]).astype(BF16)

    pre_one = dot(w1[2 * chan : (rows + 4) * chan, :], x3[:, frame_dev:])
    beside = slice(frame_dev, wide)
    for start in range(0, rows + 2, 2):
        result = dot(wb[...], rim[start * 3 * chan : (start + 4) * 3 * chan, :])
        for n in range(2):
            at = slice((start + n) * chan, (start + n + 1) * chan)
            put(start + n - 1, beside, result[n * chan : (n + 1) * chan], pre_one[at])
    own = slice(0, frame_dev)
    result = dot(wb[...], g3[: 4 * 3 * chan, :])
    put(-1, own, result[:chan], dot(w1[2 * chan : 3 * chan, :], x3[:, :frame_dev]))
    result = dot(wb[...], g3[4 * 3 * chan :, :])
    put(rows, own, result[chan:], dot(w1[(rows + 3) * chan : (rows + 4) * chan, :], x3[:, :frame_dev]))
    row = features[0:1, :]
    lane = iota((1, 128), 1)
    gram = jnp.concatenate(
        [jnp.where(lane < 9, pltpu.roll(row, 128 - 9 * t, 1) if t else row, 0.0) for t in range(9)]
        + [jnp.zeros((7, 128), F32)],
        axis=0,
    )
    single = to_column(row, 16, 81)[0:9]
    k_rows = jnp.concatenate([k1t[...], jnp.zeros((112, chan), F32)], axis=0)
    mean_l, inv_l = stats[chan : chan + 1, :chan], stats[chan + 8 : chan + 9, :chan]
    normed = inv_l * (dot(gram, k_rows, precision=EXACT)[0:9] - single * mean_l)
    normed_taps[0:16] = jnp.concatenate([normed, jnp.zeros((7, chan), F32)], axis=0)
    normed_taps[16:32] = jnp.broadcast_to(to_column(row, 16, 81), (16, chan))
    load.wait()
    first[...] = dot(ws[...], low[...])


def finish(recv, features, stats, k1t, first, ws, w1, x3, normed_taps, params, masks,
           spec_hbm, kernel_one_hbm, kernel_two_hbm, gain_hbm, bias_hbm,
           spec_grad, kernel_one, kernel_two, gain_out, bias_out, got, sems):
    chan = params.shape[1]
    rows = MEL_ROWS
    wide = x3.shape[1]
    frame_dev = wide - RIM
    usable, behind, ahead = (masks[n : n + 1] for n in range(3))
    total = masks[3:4, 0:1]
    gain = params[0:1]
    count = recv.shape[0]
    share = half_share(count, 9 * chan)
    got[...] = recv[...].astype(F32).reshape(count * LAST, 128)
    sums = summed_blocks(got, count)
    sums = sums[0:5] + sums[5:10] + sums[10:15]
    ten = jnp.concatenate([sums[:, :chan], sums[:, chan:]], axis=0)
    bias_sum = ten[9:10]
    mean_l, inv_l = stats[chan : chan + 1, :chan], stats[chan + 8 : chan + 9, :chan]
    ten = ten - features[1:2, 0:1] * bias_sum
    k = k1t[0:9]
    gain_sum = inv_l * (jnp.sum(k * ten[0:9], axis=0, keepdims=True) - mean_l * bias_sum)
    gain_out[...] = gain_sum
    bias_out[...] = bias_sum
    factor_l = gain * inv_l
    scale = factor_l * gain_sum / total * inv_l
    scale = jnp.concatenate(
        [scale * row_valid(-1, rows)] + [scale] * rows + [scale * row_valid(rows, rows)], axis=1
    )
    many = 3 * rows

    def in_parts(v, right):
        high = lax.reduce_precision(v, 8, 7)
        v = dot(jnp.concatenate([high, v - high], axis=0).astype(BF16), right)
        return v[:many] + v[many:]

    combined = in_parts(ws[...].astype(F32) * scale, w1[2 * chan : (rows + 4) * chan, :])
    left = [got[pl.ds(15 + p, count, stride=LAST), :] for p in range(share)]
    taps = TAPS // 2
    whole = [jnp.concatenate([v[:, h * chan : (h + 1) * chan] for v in left], axis=0)[:taps] for h in range(2)]
    whole = jnp.concatenate(whole, axis=0)
    for t in range(9):
        kernel_two[t] = whole[t * chan : (t + 1) * chan].T
    stores = [pltpu.make_async_copy(kernel_two, kernel_two_hbm, sems.at[4])]
    stores[0].start()
    taken = in_parts(combined, x3[...])
    taps = first[...] - taken
    moved = [taps[rows * b : rows * (b + 1)] for b in range(3)]
    mean_full = mean_l + features[1:2, 0:1] * jnp.sum(k, axis=0, keepdims=True)
    constant = jnp.sum(k * (factor_l * (bias_sum - gain_sum * inv_l * mean_full) / total), axis=1, keepdims=True)
    for a in range(3):
        row = iota((rows, 1), 0) + (a - 1) + lax.axis_index("mel") * rows
        valid = ((row >= 0) & (row < lax.axis_size("mel") * rows)).astype(F32) * usable
        for b in range(3):
            t = 3 * (2 - a) + 2 - b
            moved[b] = moved[b] - constant[t : t + 1] * valid
    result = pltpu.roll(moved[0], 1, 1) * behind + moved[1] + pltpu.roll(moved[2], wide - 1, 1) * ahead
    spec_grad[0] = (result * usable)[:, :frame_dev]
    grad_taps = factor_l * (ten[0:9] - (bias_sum * normed_taps[16:25] + gain_sum * normed_taps[0:9]) / total)
    for i in range(3):
        kernel_one[i] = grad_taps[3 * i : 3 * i + 3]
    outs = ((spec_grad, spec_hbm), (kernel_one, kernel_one_hbm), (gain_out, gain_hbm), (bias_out, bias_hbm))
    wait_all(stores + start_all(*outs, sems=sems))


def run(kernel, outs, scratch, *args, hbm=0, apart=(), flops=10**8, size=4 * 10**6):
    vmem = pl.BlockSpec(memory_space=pltpu.VMEM)
    devices = lax.axis_size("mel") * lax.axis_size("tm")
    specs = []
    args = list(args)
    for n, a in enumerate(args):
        if hbm and n >= len(args) - hbm:
            specs.append(pl.BlockSpec(memory_space=pltpu.HBM))
            args[n] = pltpu.with_memory_space_constraint(a, pltpu.HBM)
        else:
            specs.append(vmem)
            args[n] = pltpu.with_memory_space_constraint(a, pltpu.VMEM)
    return pl.pallas_call(
        kernel,
        out_shape=outs,
        in_specs=specs,
        out_specs=[pl.BlockSpec(memory_space=pltpu.HBM) if n in apart else vmem for n in range(len(outs))],
        scratch_shapes=scratch,
        compiler_params=pltpu.CompilerParams(vmem_limit_bytes=(29 + devices // 32) * 2**20),
        cost_estimate=pl.CostEstimate(flops=flops, bytes_accessed=size, transcendentals=0),
    )(*args)


def shape(dims, dtype=F32):
    return jax.ShapeDtypeStruct(dims, dtype)


def kept(dims, dtype=F32):
    return pltpu.VMEM(dims, dtype)


def far(dims, dtype=F32):
    return pltpu.HBM(dims, dtype)


def exchange(blocks, axes=AXES):
    return lax.all_to_all(blocks, axes, 0, 0, tiled=True)


def exchange_rows(rows, axes=AXES):
    return exchange(rows[:, None, :], axes)[:, 0, :]


def shards(spectrum, clip_bounds, kernel_one, gain_one, bias_one, kernel_two, gain_two, bias_two, pooled_grad):
    _, rows, frame_dev = spectrum.shape
    chan = kernel_two.shape[0]
    n_mel, n_tm = lax.axis_size("mel"), lax.axis_size("tm")
    devices = n_mel * n_tm
    half = frame_dev // 2
    wide = frame_dev + RIM
    mels = n_mel * rows

    packed, own, spec, masks = run(
        pack,
        [
            kept((devices, FIRST, 128), BF16),
            kept(pooled_grad.shape, BF16),
            kept(spectrum.shape, BF16),
            kept((8, wide)),
        ],
        [
            pltpu.VMEM(clip_bounds.shape, jnp.int32),
            pltpu.VMEM((2 * chan, half), F32),
            pltpu.VMEM((devices * FIRST, 128), F32),
            pltpu.SemaphoreType.DMA((3,)),
        ],
        spectrum,
        pooled_grad,
        clip_bounds,
        hbm=3,
    )
    recv = exchange(packed)
    ext = rows + 6
    span = 4 * 3 * chan
    wf, wb, w1, ws, pairs, singles, k1t, params, all_masks, edge_masks, twice, own_rows = run(
        weights,
        [
            kept((2 * chan, span), BF16),
            kept((2 * chan, span), BF16),
            kept((ext * chan, 128), BF16),
            far((rows * 3, (rows + 2) * chan), BF16),
            kept((chan, 128)),
            kept((chan, 128)),
            kept((16, chan)),
            kept((8, chan)),
            kept((3 * n_tm, frame_dev)),
            kept((n_tm * 8, 128)),
            kept((128, 128)),
            kept((chan * rows // 2, half), BF16),
        ],
        [
            pltpu.VMEM((9, chan, chan), BF16),
            pltpu.VMEM((3, 3, chan), BF16),
            pltpu.VMEM((4, 1, chan), F32),
            pltpu.VMEM(clip_bounds.shape, jnp.int32),
            pltpu.VMEM((rows * 3, (rows + 2) * chan), BF16),
            pltpu.VMEM((chan * rows // 2, half), F32),
            pltpu.SemaphoreType.DMA((8,)),
        ],
        own,
        clip_bounds,
        jnp.transpose(kernel_two, (2, 3, 0, 1)).reshape(9, chan, chan),
        jnp.transpose(kernel_one, (1, 2, 0)),
        gain_one[None],
        bias_one[None],
        gain_two[None],
        bias_two[None],
        hbm=7,
        apart=(3,),
    )
    pre_two, payload, act, x3, far_rim, stats_one, features = run(
        forward_one,
        [
            kept((rows * chan, wide)),
            kept((devices, SECOND, 128), BF16),
            kept((ext * 3 * chan, wide), BF16),
            kept((128, wide), BF16),
            kept((BAND, RIM)),
            kept((2 * chan + 16, 128)),
            kept((8, 128)),
        ],
        [
            pltpu.VMEM((ext * chan, wide), F32),
            pltpu.VMEM((devices * FIRST, 128), F32),
            pltpu.VMEM((n_tm * 8, 128), F32),
            pltpu.VMEM((mels + 8, RIM), F32),
            pltpu.VMEM((devices * SECOND, 128), F32),
        ],
        recv,
        spec,
        pairs,
        singles,
        twice,
        w1,
        wf,
        params,
        masks,
        all_masks,
        edge_masks,
    )
    recv = exchange(payload)
    grad, kept_half, sent_half, totals, stats_two, row_pairs = run(
        backward_scaled,
        [
            kept((rows * chan, frame_dev)),
            kept((TAPS // 2 + devices, 128)),
            kept((TAPS // 2 + devices, 128)),
            kept((8, 128)),
            kept((chan + 8, 128)),
            kept((rows // 2 * chan, frame_dev)),
        ],
        [
            pltpu.VMEM((rows // 2 * chan, frame_dev), F32),
            pltpu.VMEM((3 * chan + 16, rows * frame_dev), BF16),
            pltpu.VMEM((2, TAPS // 2 + devices, 128), F32),
        ],
        recv,
        pre_two,
        act,
        own_rows,
        params,
        masks,
    )
    received = lax.ppermute(sent_half, "tm", [(i, i ^ 1) for i in range(n_tm)])
    pre_ring, ring, rim = run(
        around,
        [kept((4 * chan, wide)), kept((4 * chan, wide)), kept((rows * chan, RIM))],
        [
            pltpu.VMEM(((rows // 2 + 2) * chan, RIM), F32),
            pltpu.VMEM((2 * chan, frame_dev), F32),
            pltpu.VMEM((devices * SECOND, 128), F32),
            pltpu.VMEM((2 * chan, half), F32),
            pltpu.VMEM((4 * 3 * chan, wide), BF16),
        ],
        recv,
        pre_two,
        act,
        w1,
        wf,
        x3,
        far_rim,
        stats_one,
        masks,
        stats_two,
    )
    (payload,) = run(
        pack_sums,
        [kept((devices * (half_share(devices, 9 * chan) + 2), 128))],
        [],
        kept_half,
        received,
        totals,
        rim,
    )
    recv = exchange_rows(payload)
    grad, own_low, payload, totals = run(
        backward,
        [
            kept(((rows + 4) * chan, wide), BF16),
            kept((rows * chan, frame_dev), BF16),
            kept((devices, LAST, 128), BF16),
            kept((8, 128)),
        ],
        [
            pltpu.VMEM(((rows + 2) * 3 * chan, frame_dev), BF16),
            pltpu.VMEM((rows * chan, frame_dev), F32),
            pltpu.VMEM((rows * chan, 2 * frame_dev), BF16),
        ],
        recv,
        pre_two,
        pre_ring,
        grad,
        ring,
        rim,
        stats_two,
        w1,
        x3,
        stats_one,
        params,
        masks,
        wb,
    )
    recv = exchange(payload)
    pooled, gain_two_grad, bias_two_grad = run(
        pool,
        [shape((1, chan, rows // 2, half), BF16), shape((1, chan)), shape((1, chan))],
        [
            pltpu.VMEM((rows // 2 * chan, 128), F32),
        ],
        totals,
        row_pairs,
    )
    first, ws, normed_taps = run(
        transposed,
        [
            kept((rows * 3, wide)),
            kept((rows * 3, (rows + 2) * chan), BF16),
            kept((32, chan)),
        ],
        [
            pltpu.VMEM(((rows + 2) * chan, wide), BF16),
            pltpu.VMEM((8 * 3 * chan, frame_dev), BF16),
            pltpu.VMEM(((rows + 4) * 3 * chan, RIM), BF16),
            pltpu.SemaphoreType.DMA,
        ],
        grad,
        own_low,
        w1,
        wb,
        x3,
        stats_one,
        features,
        k1t,
        params,
        masks,
        ws,
        hbm=1,
    )
    spec_grad, kernel_one_grad, kernel_two_grad, gain_one_grad, bias_one_grad = run(
        finish,
        [
            shape((1, rows, frame_dev)),
            shape((3, 3, chan)),
            shape((9, chan, chan)),
            shape((1, chan)),
            shape((1, chan)),
        ],
        [
            pltpu.VMEM((1, rows, frame_dev), F32),
            pltpu.VMEM((3, 3, chan), F32),
            pltpu.VMEM((9, chan, chan), F32),
            pltpu.VMEM((1, chan), F32),
            pltpu.VMEM((1, chan), F32),
            pltpu.VMEM((devices * LAST, 128), F32),
            pltpu.SemaphoreType.DMA((5,)),
        ],
        recv,
        features,
        stats_one,
        k1t,
        first,
        ws,
        w1,
        x3,
        normed_taps,
        params,
        masks,
        apart=range(5),
    )
    kernel_two_grad = jnp.transpose(kernel_two_grad.reshape(3, 3, chan, chan), (2, 3, 0, 1))
    return (
        pooled,
        spec_grad,
        jnp.transpose(kernel_one_grad, (2, 0, 1)),
        gain_one_grad[0],
        bias_one_grad[0],
        kernel_two_grad,
        gain_two_grad[0],
        bias_two_grad[0],
    )


def solution(mesh):
    return jax.shard_map(
        shards,
        mesh=mesh,
        in_specs=(
            P(None, "mel", "tm"),
            P(),
            P(),
            P(),
            P(),
            P(),
            P(),
            P(),
            P(None, None, "mel", "tm"),
        ),
        out_specs=(P(None, None, "mel", "tm"), P(None, "mel", "tm"), P(), P(), P(), P(), P(), P()),
        check_vma=False,
    )
```
